32 devices in a mesh: dp: 4 (over y, x), seq: 8 (over z, core).
Axes of the slice: x: 2, y: 2, z: 4, core: 2. Of those that a mesh axis runs over, the one named last changes fastest.
Arguments:
- tokens_in: bfloat16 [4, 1024, 768], P('dp', 'seq'), may hold values from -6 to 6
- cotangent: bfloat16 [4, 1024, 768], P('dp', 'seq'), may hold values from -6 to 6
- timesteps: int32 [4], P('dp'), may hold values from 0 to 999
- span_start: int32 [4], P('dp'), may hold values from 0 to 1023
- span_len: int32 [4], P('dp'), may hold values from 1 to 512
- vectors: float32 [9, 768], replicated, may hold values from -4 to 4, as said below
- w_ada: float32 [128, 4608], P(None, ('dp', 'seq')), may hold values from -0.5 to 0.5
- w_qkv: float32 [768, 2304], P(('dp', 'seq')), may hold values from -0.21875 to 0.21875
- w_attn: float32 [768, 768], P(('dp', 'seq')), may hold values from -3 to 3
- w_in: float32 [768, 3072], P(('dp', 'seq')), may hold values from -0.21875 to 0.21875
- w_out: float32 [3072, 768], P(('dp', 'seq')), may hold values from -0.109375 to 0.109375
- m_vec: float32 [9, 768], P(None, ('dp', 'seq')), may hold values from -0.0017089844 to 0.0017089844
- v_vec: float32 [9, 768], P(None, ('dp', 'seq')), may hold values from 1.1726959e-09 to 4.6907838e-09
- m_ada: float32 [128, 4608], P(None, ('dp', 'seq')), may hold values from -0.00061035156 to 0.00061035156
- v_ada: float32 [128, 4608], P(None, ('dp', 'seq')), may hold values from 1.3029955e-10 to 5.211982e-10
- m_qkv: float32 [768, 2304], P(('dp', 'seq')), may hold values from -0.00061035156 to 0.00061035156
- v_qkv: float32 [768, 2304], P(('dp', 'seq')), may hold values from 1.3029955e-10 to 5.211982e-10
- m_attn: float32 [768, 768], P(('dp', 'seq')), may hold values from -0.00061035156 to 0.00061035156
- v_attn: float32 [768, 768], P(('dp', 'seq')), may hold values from 1.3029955e-10 to 5.211982e-10
- m_in: float32 [768, 3072], P(('dp', 'seq')), may hold values from -0.00061035156 to 0.00061035156
- v_in: float32 [768, 3072], P(('dp', 'seq')), may hold values from 1.3029955e-10 to 5.211982e-10
- m_out: float32 [3072, 768], P(('dp', 'seq')), may hold values from -0.00061035156 to 0.00061035156
- v_out: float32 [3072, 768], P(('dp', 'seq')), may hold values from 1.3029955e-10 to 5.211982e-10
Outputs:
- block_out: bfloat16 [4, 1024, 768], P('dp', 'seq')
- grad_input: float32 [4, 1024, 768], P('dp', 'seq')
- grad_norm: float32 [], replicated
- vec_first: float32 [9, 768], P(None, ('dp', 'seq'))
- vec_second: float32 [9, 768], P(None, ('dp', 'seq'))
- vec_new: float32 [9, 768], P(None, ('dp', 'seq'))
- ada_first: float32 [128, 4608], P(None, ('dp', 'seq'))
- ada_second: float32 [128, 4608], P(None, ('dp', 'seq'))
- ada_new: float32 [128, 4608], P(None, ('dp', 'seq'))
- qkv_first: float32 [768, 2304], P(('dp', 'seq'))
- qkv_second: float32 [768, 2304], P(('dp', 'seq'))
- qkv_new: float32 [768, 2304], P(('dp', 'seq'))
- attn_first: float32 [768, 768], P(('dp', 'seq'))
- attn_second: float32 [768, 768], P(('dp', 'seq'))
- attn_new: float32 [768, 768], P(('dp', 'seq'))
- in_first: float32 [768, 3072], P(('dp', 'seq'))
- in_second: float32 [768, 3072], P(('dp', 'seq'))
- in_new: float32 [768, 3072], P(('dp', 'seq'))
- out_first: float32 [3072, 768], P(('dp', 'seq'))
- out_second: float32 [3072, 768], P(('dp', 'seq'))
- out_new: float32 [3072, 768], P(('dp', 'seq'))
The draws below stay inside these ranges and needn't reach their ends.
Inputs may be any that keep to these rules, and one draw needn't show every extreme that they name: Rows 0 and 1 are the gains of the two norms, rows 2 to 7 the biases of the six modulation vectors in their order, row 8 the mask embedding.
All inputs are finite; a program needn't handle non-finite values.
Results may differ from the reference program's by a relative error of at most 0.02.
Values may be sent and summed in bfloat16 or wider, within the bound.
A program may use at most 192 MiB of HBM per device.

```python
import math
import jax
import jax.numpy as jnp
from jax import lax

D = 768
H = 12
HD = 64
FF = 3072
COND = 128
STEP = 10
BATCH = 4
LEN = 1024
NPARAM = 7674624


def draw_vectors(key, part):
    key = jax.random.fold_in(key, 7)
    jitter_key, bias_key, mask_key = jax.random.split(key, 3)
    ramp = jnp.arange(D, dtype=jnp.float32) / (D - 1)
    jitter = jax.random.uniform(jitter_key, (2, D), jnp.float32, 0.8, 1.25)
    low_end = 0.6
    high_end = 1.8
    biases = 0.2 * jax.random.normal(bias_key, (6, D), jnp.float32)
    embed = jnp.clip(1.5 * jax.random.normal(mask_key, (1, D), jnp.float32), -4.0, 4.0)
    gains = low_end * (high_end / low_end) ** ramp[None, :] * jitter
    gate_rows = jnp.array([0.0, 0.0, 1.0, 0.0, 0.0, 1.0], jnp.float32)[:, None]
    return jnp.concatenate([gains, biases + gate_rows, embed], axis=0)


def plant(values, own_key, least, top_value):
    longest = values.shape.index(max(values.shape))
    spots = []
    for shift in (0, 1):
        where = [jax.random.randint(jax.random.fold_in(own_key, axis), (), 0, length) for axis, length in enumerate(values.shape)]
        where[longest] = (where[longest] + shift) % values.shape[longest]
        spots.append(tuple(where))
    return values.at[spots[0]].set(least).at[spots[1]].set(top_value)


def block_scale(rng, shape, shards, smallest, largest):
    loudness = 1.0
    for dim, blocks in shards:
        steps = jax.random.uniform(jax.random.fold_in(jax.random.fold_in(rng, 6), dim), (blocks,), jnp.float32, smallest / len(shards), largest / len(shards))
        loudness = loudness * jnp.repeat(jnp.exp(steps), shape[dim] // blocks).reshape((-1,) + (1,) * (len(shape) - 1 - dim))
    return loudness


def bell_draw(rng, extent, deviation, most, pieces=(), held_as=jnp.bfloat16):
    entries = deviation * jax.random.normal(rng, extent, jnp.float32)
    if pieces:
        entries = entries * block_scale(rng, extent, pieces, -0.22, 0.18)
    return jnp.clip(entries, -most, most).astype(held_as)


def setup_inputs(seed: int = 0) -> dict:
    arg_keys = jax.random.split(jax.random.key(seed), 24)
    tokens_in = bell_draw(arg_keys[0], (BATCH, LEN, D), 1.0, 6.0, ((0, 4), (1, 8)))
    cotangent = bell_draw(arg_keys[1], (BATCH, LEN, D), 1.0, 6.0, ((0, 4), (1, 8)))
    timesteps = plant(jax.random.randint(arg_keys[2], (BATCH,), 0, 1000), jax.random.fold_in(arg_keys[2], 1), 0, 999).astype(jnp.int32)
    span_start = plant(jax.random.randint(arg_keys[3], (BATCH,), 0, LEN), jax.random.fold_in(arg_keys[3], 1), 0, LEN - 1).astype(jnp.int32)
    span_len = plant(jax.random.randint(arg_keys[4], (BATCH,), 1, LEN // 2 + 1), jax.random.fold_in(arg_keys[4], 1), 1, (LEN // 2 + 1) - 1).astype(jnp.int32)
    vectors = draw_vectors(jax.random.fold_in(arg_keys[23], 71), 0)
    w_ada = bell_draw(arg_keys[6], (COND, 6 * D), COND ** -0.5, 0.5, ((1, 32),), jnp.float32)
    w_qkv = bell_draw(arg_keys[7], (D, 3 * D), D ** -0.5, 0.21875, ((0, 32),), jnp.float32)
    w_attn = bell_draw(arg_keys[8], (D, D), (0.18 * LEN ** 0.5 * D ** -0.5), 3.0, ((0, 32),), jnp.float32)
    w_in = bell_draw(arg_keys[9], (D, FF), D ** -0.5, 0.21875, ((0, 32),), jnp.float32)
    w_out = bell_draw(arg_keys[10], (FF, D), FF ** -0.5, 0.109375, ((0, 32),), jnp.float32)
    m_vec = bell_draw(arg_keys[11], (9, D), (0.33 * NPARAM ** -0.5), 0.0017089844, ((1, 32),), jnp.float32)
    v_vec = jnp.clip(jnp.exp(math.log(4.6907837614185155e-09) - 1.3862944 * jax.random.uniform(arg_keys[12], (9, D), jnp.float32) ** block_scale(arg_keys[12], (9, D), ((1, 32),), -0.2, 0.2)), 1.1726959403546289e-09, 4.6907837614185155e-09)
    m_ada = bell_draw(arg_keys[13], (COND, 6 * D), (0.11 * NPARAM ** -0.5), 0.00061035156, ((1, 32),), jnp.float32)
    v_ada = jnp.clip(jnp.exp(math.log(5.211981957131684e-10) - 1.3862944 * jax.random.uniform(arg_keys[14], (COND, 6 * D), jnp.float32) ** block_scale(arg_keys[14], (COND, 6 * D), ((1, 32),), -0.2, 0.2)), 1.302995489282921e-10, 5.211981957131684e-10)
    m_qkv = bell_draw(arg_keys[15], (D, 3 * D), (0.11 * NPARAM ** -0.5), 0.00061035156, ((0, 32),), jnp.float32)
    v_qkv = jnp.clip(jnp.exp(math.log(5.211981957131684e-10) - 1.3862944 * jax.random.uniform(arg_keys[16], (D, 3 * D), jnp.float32) ** block_scale(arg_keys[16], (D, 3 * D), ((0, 32),), -0.2, 0.2)), 1.302995489282921e-10, 5.211981957131684e-10)
    m_attn = bell_draw(arg_keys[17], (D, D), (0.11 * NPARAM ** -0.5), 0.00061035156, ((0, 32),), jnp.float32)
    v_attn = jnp.clip(jnp.exp(math.log(5.211981957131684e-10) - 1.3862944 * jax.random.uniform(arg_keys[18], (D, D), jnp.float32) ** block_scale(arg_keys[18], (D, D), ((0, 32),), -0.2, 0.2)), 1.302995489282921e-10, 5.211981957131684e-10)
    m_in = bell_draw(arg_keys[19], (D, FF), (0.11 * NPARAM ** -0.5), 0.00061035156, ((0, 32),), jnp.float32)
    v_in = jnp.clip(jnp.exp(math.log(5.211981957131684e-10) - 1.3862944 * jax.random.uniform(arg_keys[20], (D, FF), jnp.float32) ** block_scale(arg_keys[20], (D, FF), ((0, 32),), -0.2, 0.2)), 1.302995489282921e-10, 5.211981957131684e-10)
    m_out = bell_draw(arg_keys[21], (FF, D), (0.11 * NPARAM ** -0.5), 0.00061035156, ((0, 32),), jnp.float32)
    v_out = jnp.clip(jnp.exp(math.log(5.211981957131684e-10) - 1.3862944 * jax.random.uniform(arg_keys[22], (FF, D), jnp.float32) ** block_scale(arg_keys[22], (FF, D), ((0, 32),), -0.2, 0.2)), 1.302995489282921e-10, 5.211981957131684e-10)
    return dict(tokens_in=tokens_in, cotangent=cotangent, timesteps=timesteps, span_start=span_start, span_len=span_len, vectors=vectors, w_ada=w_ada, w_qkv=w_qkv, w_attn=w_attn, w_in=w_in, w_out=w_out, m_vec=m_vec, v_vec=v_vec, m_ada=m_ada, v_ada=v_ada, m_qkv=m_qkv, v_qkv=v_qkv, m_attn=m_attn, v_attn=v_attn, m_in=m_in, v_in=v_in, m_out=m_out, v_out=v_out)


@jax.custom_vjp
def low(v):
    return lax.optimization_barrier(v.astype(jnp.bfloat16)).astype(jnp.float32)

@jax.custom_vjp
def low_back(v):
    return v

def low_keep(v):
    return (low(v), None)

def low_pass(kept, grad):
    return (grad,)

def back_keep(v):
    return (v, None)

def back_low(kept, grad):
    return (low(grad),)
low.defvjp(low_keep, low_pass)
low_back.defvjp(back_keep, back_low)
HIGH = lax.Precision.HIGHEST
BETA_ONE = 0.9
BETA_TWO = 0.999
ADAM_EPS = 1e-08
RATE = 0.1
RATE_VECTORS = 0.3
DECAY = 0.01
CLIP = 1.0
NORM_EPS = 1e-05

def cond_input(timesteps):
    half_cond = COND // 2
    freqs = jnp.exp(jnp.arange(half_cond, dtype=jnp.float32) * (-math.log(10000.0) / half_cond))
    angles = timesteps.astype(jnp.float32)[:, None] * freqs[None, :]
    return jax.nn.silu(jnp.concatenate([jnp.cos(angles), jnp.sin(angles)], axis=1))

def rotary_tables(positions):
    half_head = HD // 2
    inverse = jnp.exp(jnp.arange(half_head, dtype=jnp.float32) * (-math.log(10000.0) / half_head))
    angles = positions.astype(jnp.float32)[:, None] * inverse[None, :]
    return (jnp.cos(angles), jnp.sin(angles))

def rotate(values, cosines, sines):
    half_head = values.shape[-1] // 2
    first = values[..., :half_head]
    second = values[..., half_head:]
    cos_b = cosines[:, None, :]
    sin_b = sines[:, None, :]
    return jnp.concatenate([first * cos_b - second * sin_b, second * cos_b + first * sin_b], axis=-1)

def layer_norm(values):
    centre = lax.optimization_barrier(jnp.mean(values, axis=-1, keepdims=True))
    centred = values - centre
    return centred * lax.rsqrt(lax.optimization_barrier(jnp.mean(centred * centred, axis=-1, keepdims=True)) + NORM_EPS)

def one_sequence(params, items):
    vectors, w_ada, w_qkv, w_attn, w_in, w_out = params
    tokens, masked, cond = items
    modulation = jnp.dot(low(cond)[None, :], w_ada, precision=HIGH)[0] + vectors[2:8].reshape(6 * D)
    parts = modulation.reshape(6, D)
    shift_one, scale_one, gate_one = (parts[0], parts[1], parts[2])
    shift_two, scale_two, gate_two = (parts[3], parts[4], parts[5])
    start_tokens = jnp.where(masked[:, None], vectors[8][None, :], tokens)
    hidden_one = low(layer_norm(start_tokens) * vectors[0] * (1.0 + scale_one) + shift_one)
    projected = low_back(jnp.dot(hidden_one, w_qkv, precision=HIGH))
    cosines, sines = rotary_tables(jnp.arange(LEN, dtype=jnp.int32))
    queries = low(rotate(projected[:, :D].reshape(LEN, H, HD), cosines, sines))
    keys_all = low(rotate(projected[:, D:2 * D].reshape(LEN, H, HD), cosines, sines))
    values_all = low(projected[:, 2 * D:].reshape(LEN, H, HD))
    block_rows = math.gcd(LEN, 512)
    factor = HD ** (-0.5)

    def attend(query_block):
        scores = jnp.einsum('qhd,khd->hqk', query_block, keys_all, precision=HIGH) * factor
        scores = low_back(scores)
        probs = jax.nn.softmax(scores, axis=-1)
        return jnp.einsum('hqk,khd->qhd', low(probs), values_all, precision=HIGH)
    attended = lax.map(jax.checkpoint(attend), queries.reshape(LEN // block_rows, block_rows, H, HD))
    attended = attended.reshape(LEN, D)
    branch_one = low_back(jnp.dot(low(low_back(attended)), w_attn, precision=HIGH))
    mid_tokens = start_tokens + gate_one * branch_one
    hidden_two = low(layer_norm(mid_tokens) * vectors[1] * (1.0 + scale_two) + shift_two)
    pre_act = low_back(jnp.dot(hidden_two, w_in, precision=HIGH))
    activ = low(jax.nn.gelu(pre_act, approximate=True))
    branch_two = low_back(jnp.dot(activ, w_out, precision=HIGH))
    return mid_tokens + gate_two * branch_two

def adam_step(weight, grad, first, second, rate, decay_rate):
    new_first = BETA_ONE * first + (1.0 - BETA_ONE) * grad
    new_second = BETA_TWO * second + (1.0 - BETA_TWO) * grad * grad
    fixed_first = new_first / (1.0 - BETA_ONE ** STEP)
    fixed_second = new_second / (1.0 - BETA_TWO ** STEP)
    new_weight = weight - rate * (fixed_first / (jnp.sqrt(fixed_second) + ADAM_EPS) + decay_rate * weight)
    return (new_first, new_second, new_weight)

def reference(tokens_in, cotangent, timesteps, span_start, span_len, vectors, w_ada, w_qkv, w_attn, w_in, w_out, m_vec, v_vec, m_ada, v_ada, m_qkv, v_qkv, m_attn, v_attn, m_in, v_in, m_out, v_out):
    positions = jnp.arange(LEN, dtype=jnp.int32)
    masked = (positions[None, :] >= span_start[:, None]) & (positions[None, :] < (span_start + span_len)[:, None])
    cond = cond_input(timesteps)

    def run(params, tokens):
        vecs, ada, qkv, attn, inner, outer = params
        rounded = (vecs, low(ada), low(qkv), low(attn), low(inner), low(outer))

        def per_seq(items):
            return one_sequence(rounded, items)
        return lax.map(jax.checkpoint(per_seq), (tokens, masked, cond))
    params = (vectors, w_ada, w_qkv, w_attn, w_in, w_out)
    result, back = jax.vjp(run, params, tokens_in.astype(jnp.float32))
    grads, grad_tokens = back(cotangent.astype(jnp.float32))
    squares = jnp.float32(0.0)
    for grad in grads:
        squares = squares + jnp.sum(grad * grad)
    grad_norm = jnp.sqrt(squares)
    clip_factor = jnp.minimum(1.0, CLIP / (grad_norm + 1e-06))
    g_vec, g_ada, g_qkv, g_attn, g_in, g_out = [grad * clip_factor for grad in grads]
    vec_out = adam_step(vectors, g_vec, m_vec, v_vec, RATE_VECTORS, 0.0)
    ada_out = adam_step(w_ada, g_ada, m_ada, v_ada, RATE, DECAY)
    qkv_out = adam_step(w_qkv, g_qkv, m_qkv, v_qkv, RATE, DECAY)
    attn_out = adam_step(w_attn, g_attn, m_attn, v_attn, RATE, DECAY)
    in_out = adam_step(w_in, g_in, m_in, v_in, RATE, DECAY)
    out_out = adam_step(w_out, g_out, m_out, v_out, RATE, DECAY)
    return (result.astype(jnp.bfloat16), grad_tokens, grad_norm, vec_out[0], vec_out[1], vec_out[2], ada_out[0], ada_out[1], ada_out[2], qkv_out[0], qkv_out[1], qkv_out[2], attn_out[0], attn_out[1], attn_out[2], in_out[0], in_out[1], in_out[2], out_out[0], out_out[1], out_out[2])
```

```python
from functools import partial
import math
from types import SimpleNamespace

import jax
import jax.numpy as jnp
from jax import lax
from jax.experimental import pallas as pl
from jax.experimental.pallas import tpu as pltpu
from jax.sharding import PartitionSpec as P

HD = 64
COND = 128
STEP = 10


BETA_ONE = 0.9
BETA_TWO = 0.999
ADAM_EPS = 1e-08
RATE = 0.1
RATE_VECTORS = 0.3
DECAY = 0.01
CLIP = 1.0
NORM_EPS = 1e-05


def cond_input(timesteps):
    half_cond = COND // 2
    freqs = jnp.exp(jnp.arange(half_cond, dtype=jnp.float32) * (-math.log(10000.0) / half_cond))
    angles = timesteps.astype(jnp.float32)[:, None] * freqs[None, :]
    return jax.nn.silu(jnp.concatenate([jnp.cos(angles), jnp.sin(angles)], axis=1))


def rotary_tables(positions):
    half_head = HD // 2
    inverse = jnp.exp(jnp.arange(half_head, dtype=jnp.float32) * (-math.log(10000.0) / half_head))
    angles = positions.astype(jnp.float32)[:, None] * inverse[None, :]
    return (jnp.cos(angles), jnp.sin(angles))


def rotate(values, cosines, sines):
    half_head = values.shape[-1] // 2
    first = values[..., :half_head]
    second = values[..., half_head:]
    cos_b = cosines[:, None, :]
    sin_b = sines[:, None, :]
    return jnp.concatenate(
        [first * cos_b - second * sin_b, second * cos_b + first * sin_b], axis=-1
    )


def rotate_back(grads, cosines, sines):
    half_head = grads.shape[-1] // 2
    first = grads[..., :half_head]
    second = grads[..., half_head:]
    cos_b = cosines[:, None, :]
    sin_b = sines[:, None, :]
    return jnp.concatenate(
        [first * cos_b + second * sin_b, second * cos_b - first * sin_b], axis=-1
    )


def normalize(values):
    centre = jnp.mean(values, axis=-1, keepdims=True)
    centred = values - centre
    inverse = lax.rsqrt(jnp.mean(centred * centred, axis=-1, keepdims=True) + NORM_EPS)
    return (centred * inverse, inverse)


def norm_back(normed, inverse, grad):
    return inverse * (
        grad
        - jnp.mean(grad, axis=-1, keepdims=True)
        - normed * jnp.mean(grad * normed, axis=-1, keepdims=True)
    )


def split_kv(block, width):
    seqs, block_rows = (block.shape[0], block.shape[1])
    keys = block[..., :width].reshape(seqs, block_rows, width // HD, HD)
    values = block[..., width:].reshape(seqs, block_rows, width // HD, HD)
    return (keys, values)


def attend_piece(carry, piece, queries, width, factor):
    piece_rows = piece.shape[1]
    size = math.gcd(piece_rows, 512)

    def attend_one_block(index, state):
        running, denom, accum = state
        block = lax.dynamic_slice_in_dim(piece, index * size, size, 1)
        keys, values = split_kv(block, width)
        scores = (
            jnp.einsum("sqhd,skhd->shqk", queries, keys, preferred_element_type=jnp.float32)
            * factor
        )
        highest = jnp.maximum(running, jnp.max(scores, axis=-1))
        shrink = jnp.exp(running - highest)
        weights = jnp.exp(scores - highest[..., None])
        denom = denom * shrink + jnp.sum(weights, axis=-1)
        accum = accum * shrink[..., None] + jnp.einsum(
            "shqk,skhd->shqd",
            weights.astype(jnp.bfloat16),
            values,
            preferred_element_type=jnp.float32,
        )
        return (highest, denom, accum)

    return lax.fori_loop(0, piece_rows // size, attend_one_block, carry)


def block_grads(block, queries, grad_out, logsum, delta, width, factor):
    keys, values = split_kv(block, width)
    scores = (
        jnp.einsum("sqhd,skhd->shqk", queries, keys, preferred_element_type=jnp.float32) * factor
    )
    probs = jnp.exp(scores - logsum[..., None])
    dprobs = jnp.einsum("sqhd,skhd->shqk", grad_out, values, preferred_element_type=jnp.float32)
    dscores = (probs * (dprobs - delta[..., None])).astype(jnp.bfloat16)
    return (keys, probs, dscores)


def query_grads(kv_all, queries, grad_out, logsum, delta, width, factor):
    total_rows = kv_all.shape[1]
    size = math.gcd(total_rows, 512)

    def query_one_block(index, accum):
        block = lax.dynamic_slice_in_dim(kv_all, index * size, size, 1)
        keys, probs, dscores = block_grads(block, queries, grad_out, logsum, delta, width, factor)
        return accum + factor * jnp.einsum(
            "shqk,skhd->sqhd", dscores, keys, preferred_element_type=jnp.float32
        )

    return lax.fori_loop(
        0, total_rows // size, query_one_block, jnp.zeros(queries.shape, jnp.float32)
    )


def key_grads(kv_all, queries, grad_out, logsum, delta, width, factor, count):
    size = math.gcd(count, 512)
    seqs = queries.shape[0]

    def key_one_block(index, accum):
        block = lax.dynamic_slice_in_dim(kv_all, index * size, size, 1)
        keys, probs, dscores = block_grads(block, queries, grad_out, logsum, delta, width, factor)
        grad_vals = jnp.einsum(
            "shqk,sqhd->skhd",
            probs.astype(jnp.bfloat16),
            grad_out,
            preferred_element_type=jnp.float32,
        )
        grad_keys = factor * jnp.einsum(
            "shqk,sqhd->skhd", dscores, queries, preferred_element_type=jnp.float32
        )
        joined = jnp.concatenate(
            [grad_keys.reshape(seqs, size, width), grad_vals.reshape(seqs, size, width)], axis=-1
        )
        return lax.dynamic_update_slice_in_dim(
            accum, jnp.transpose(joined, (1, 0, 2)), index * size, 0
        )

    initial = jnp.zeros((count, seqs, 2 * width), jnp.float32)
    return lax.fori_loop(0, count // size, key_one_block, initial)


def adam_step(weight, grad, first, second, rate, decay_rate):
    new_first = BETA_ONE * first + (1.0 - BETA_ONE) * grad
    new_second = BETA_TWO * second + (1.0 - BETA_TWO) * grad * grad
    fixed_first = new_first / (1.0 - BETA_ONE**STEP)
    fixed_second = new_second / (1.0 - BETA_TWO**STEP)
    new_weight = weight - rate * (
        fixed_first / (jnp.sqrt(fixed_second) + ADAM_EPS) + decay_rate * weight
    )
    return (new_first, new_second, new_weight)


def mod_back(grad_hidden, ln_values, normed, scale_part, gain):
    grad_shift = jnp.sum(grad_hidden, axis=1)
    grad_scale = jnp.sum(grad_hidden * ln_values, axis=1)
    grad_ln = grad_hidden * (1.0 + scale_part)
    grad_gain = jnp.sum(grad_ln * normed, axis=(0, 1))
    return (grad_shift, grad_scale, grad_gain, grad_ln * gain)


def plain(
    tokens_in,
    cotangent,
    timesteps,
    span_start,
    span_len,
    vectors,
    w_ada,
    w_qkv,
    w_attn,
    w_in,
    w_out,
    m_vec,
    v_vec,
    m_ada,
    v_ada,
    m_qkv,
    v_qkv,
    m_attn,
    v_attn,
    m_in,
    v_in,
    m_out,
    v_out,
):
    seqs, group, width = tokens_in.shape
    heads = width // HD
    factor = HD ** (-0.5)
    flat_rows = seqs * group
    full_ada, full_qkv, full_attn, full_in, full_out = (
        lax.all_gather(w_ada.astype(jnp.bfloat16), ("dp", "seq"), axis=1, tiled=True),
        lax.all_gather(w_qkv.astype(jnp.bfloat16), ("dp", "seq"), axis=0, tiled=True),
        lax.all_gather(w_attn.astype(jnp.bfloat16), ("dp", "seq"), axis=0, tiled=True),
        lax.all_gather(w_in.astype(jnp.bfloat16), ("dp", "seq"), axis=0, tiled=True),
        lax.all_gather(w_out.astype(jnp.bfloat16), ("dp", "seq"), axis=0, tiled=True),
    )
    positions = lax.axis_index("seq") * group + jnp.arange(group, dtype=jnp.int32)
    masked = (positions[None, :] >= span_start[:, None]) & (
        positions[None, :] < (span_start + span_len)[:, None]
    )
    cond_bf = cond_input(timesteps).astype(jnp.bfloat16)
    modulation = jnp.dot(cond_bf, full_ada, preferred_element_type=jnp.float32) + vectors[
        2:8
    ].reshape(1, 6 * width)
    pieces = [modulation[:, which * width : (which + 1) * width][:, None, :] for which in range(6)]
    shift_one, scale_one, gate_one, shift_two, scale_two, gate_two = pieces
    start_tokens = jnp.where(
        masked[..., None], vectors[8][None, None, :], tokens_in.astype(jnp.float32)
    )
    normed_one, inv_one = normalize(start_tokens)
    ln_one = normed_one * vectors[0]
    hidden_one = (
        (ln_one * (1.0 + scale_one) + shift_one).astype(jnp.bfloat16).reshape(flat_rows, width)
    )
    projected = jnp.dot(hidden_one, full_qkv, preferred_element_type=jnp.float32).reshape(
        seqs, group, 3 * width
    )
    cosines, sines = rotary_tables(positions)
    queries = rotate(projected[..., :width].reshape(seqs, group, heads, HD), cosines, sines).astype(
        jnp.bfloat16
    )
    keys_here = rotate(
        projected[..., width : 2 * width].reshape(seqs, group, heads, HD), cosines, sines
    ).astype(jnp.bfloat16)
    values_here = projected[..., 2 * width :].astype(jnp.bfloat16)
    kv_local = jnp.concatenate([keys_here.reshape(seqs, group, width), values_here], axis=-1)
    initial = (
        jnp.full((seqs, heads, group), -1e30, jnp.float32),
        jnp.zeros((seqs, heads, group), jnp.float32),
        jnp.zeros((seqs, heads, group, HD), jnp.float32),
    )
    running, denom, accum = attend_piece(
        initial, lax.all_gather(kv_local, "seq", axis=1, tiled=True), queries, width, factor
    )
    attn_heads = accum / denom[..., None]
    logsum = running + jnp.log(denom)
    attn_rows = jnp.transpose(attn_heads, (0, 2, 1, 3)).reshape(flat_rows, width)
    attn_bf = attn_rows.astype(jnp.bfloat16)
    branch_one = jnp.dot(attn_bf, full_attn, preferred_element_type=jnp.float32).reshape(
        seqs, group, width
    )
    mid_tokens = start_tokens + gate_one * branch_one
    normed_two, inv_two = normalize(mid_tokens)
    ln_two = normed_two * vectors[1]
    hidden_two = (
        (ln_two * (1.0 + scale_two) + shift_two).astype(jnp.bfloat16).reshape(flat_rows, width)
    )
    pre_act = jnp.dot(hidden_two, full_in, preferred_element_type=jnp.float32)
    activ, gelu_back = jax.vjp(partial(jax.nn.gelu, approximate=True), pre_act)
    activ_bf = activ.astype(jnp.bfloat16)
    branch_two = jnp.dot(activ_bf, full_out, preferred_element_type=jnp.float32).reshape(
        seqs, group, width
    )
    block_out = (mid_tokens + gate_two * branch_two).astype(jnp.bfloat16)
    grad_y = cotangent.astype(jnp.float32)
    grad_gate_two = jnp.sum(grad_y * branch_two, axis=1)
    grad_branch_two = (grad_y * gate_two).astype(jnp.bfloat16).reshape(flat_rows, width)
    grad_w_out = jnp.dot(activ_bf.T, grad_branch_two, preferred_element_type=jnp.float32)
    grad_activ = jnp.dot(grad_branch_two, full_out.T, preferred_element_type=jnp.float32)
    grad_pre = gelu_back(grad_activ)[0].astype(jnp.bfloat16)
    grad_w_in = jnp.dot(hidden_two.T, grad_pre, preferred_element_type=jnp.float32)
    grad_hidden_two = jnp.dot(grad_pre, full_in.T, preferred_element_type=jnp.float32).reshape(
        seqs, group, width
    )
    grad_shift_two, grad_scale_two, grad_gain_two, grad_normed_two = mod_back(
        grad_hidden_two, ln_two, normed_two, scale_two, vectors[1]
    )
    grad_mid = grad_y + norm_back(normed_two, inv_two, grad_normed_two)
    grad_gate_one = jnp.sum(grad_mid * branch_one, axis=1)
    grad_branch_one = (grad_mid * gate_one).astype(jnp.bfloat16).reshape(flat_rows, width)
    grad_w_attn = jnp.dot(attn_bf.T, grad_branch_one, preferred_element_type=jnp.float32)
    grad_attn_bf = (
        jnp.dot(grad_branch_one, full_attn.T, preferred_element_type=jnp.float32)
        .astype(jnp.bfloat16)
        .reshape(seqs, group, heads, HD)
    )
    delta = jnp.einsum("sqhd,shqd->shq", grad_attn_bf.astype(jnp.float32), attn_heads)
    kv_all = lax.all_gather(kv_local, "seq", axis=1, tiled=True)
    grad_queries = query_grads(kv_all, queries, grad_attn_bf, logsum, delta, width, factor)
    grad_kv = jnp.transpose(
        lax.psum_scatter(
            key_grads(
                kv_all,
                queries,
                grad_attn_bf,
                logsum,
                delta,
                width,
                factor,
                group * lax.axis_size("seq"),
            ).astype(jnp.bfloat16),
            "seq",
            scatter_dimension=0,
            tiled=True,
        ).astype(jnp.float32),
        (1, 0, 2),
    )
    grad_keys = grad_kv[..., :width].reshape(seqs, group, heads, HD)
    grad_qkv = jnp.concatenate(
        [
            rotate_back(grad_queries, cosines, sines).reshape(seqs, group, width),
            rotate_back(grad_keys, cosines, sines).reshape(seqs, group, width),
            grad_kv[..., width:],
        ],
        axis=-1,
    )
    grad_qkv = grad_qkv.astype(jnp.bfloat16).reshape(flat_rows, 3 * width)
    grad_w_qkv = jnp.dot(hidden_one.T, grad_qkv, preferred_element_type=jnp.float32)
    grad_hidden_one = jnp.dot(grad_qkv, full_qkv.T, preferred_element_type=jnp.float32).reshape(
        seqs, group, width
    )
    grad_shift_one, grad_scale_one, grad_gain_one, grad_normed_one = mod_back(
        grad_hidden_one, ln_one, normed_one, scale_one, vectors[0]
    )
    grad_start = grad_mid + norm_back(normed_one, inv_one, grad_normed_one)
    grad_mask_row = jnp.sum(jnp.where(masked[..., None], grad_start, 0.0), axis=(0, 1))
    grad_input = jnp.where(masked[..., None], 0.0, grad_start)
    grad_mod = jnp.concatenate(
        [
            grad_shift_one,
            grad_scale_one,
            grad_gate_one,
            grad_shift_two,
            grad_scale_two,
            grad_gate_two,
        ],
        axis=1,
    )
    grad_w_ada = jnp.dot(cond_bf.astype(jnp.float32).T, grad_mod, precision=lax.Precision.HIGHEST)
    grad_vectors = jnp.concatenate(
        [
            grad_gain_one[None, :],
            grad_gain_two[None, :],
            jnp.sum(grad_mod, axis=0).reshape(6, width),
            grad_mask_row[None, :],
        ],
        axis=0,
    )
    red_ada, red_qkv, red_attn, red_in, red_out, red_vec = (
        lax.psum_scatter(grad_w_ada, ("dp", "seq"), scatter_dimension=1, tiled=True),
        lax.psum_scatter(grad_w_qkv, ("dp", "seq"), scatter_dimension=0, tiled=True),
        lax.psum_scatter(grad_w_attn, ("dp", "seq"), scatter_dimension=0, tiled=True),
        lax.psum_scatter(grad_w_in, ("dp", "seq"), scatter_dimension=0, tiled=True),
        lax.psum_scatter(grad_w_out, ("dp", "seq"), scatter_dimension=0, tiled=True),
        lax.psum_scatter(grad_vectors, ("dp", "seq"), scatter_dimension=1, tiled=True),
    )
    local_squares = jnp.float32(0.0)
    for reduced in (red_vec, red_ada, red_qkv, red_attn, red_in, red_out):
        local_squares = local_squares + jnp.sum(reduced * reduced)
    grad_norm = jnp.sqrt(lax.psum(local_squares, ("dp", "seq")))
    clip_factor = jnp.minimum(1.0, CLIP / (grad_norm + 1e-06))
    columns = red_vec.shape[1]
    own_vectors = lax.dynamic_slice_in_dim(
        vectors, lax.axis_index(("dp", "seq")) * columns, columns, 1
    )
    vec_out = adam_step(own_vectors, red_vec * clip_factor, m_vec, v_vec, RATE_VECTORS, 0.0)
    ada_out = adam_step(w_ada, red_ada * clip_factor, m_ada, v_ada, RATE, DECAY)
    qkv_out = adam_step(w_qkv, red_qkv * clip_factor, m_qkv, v_qkv, RATE, DECAY)
    attn_out = adam_step(w_attn, red_attn * clip_factor, m_attn, v_attn, RATE, DECAY)
    in_out = adam_step(w_in, red_in * clip_factor, m_in, v_in, RATE, DECAY)
    out_out = adam_step(w_out, red_out * clip_factor, m_out, v_out, RATE, DECAY)
    return (
        block_out,
        grad_input,
        grad_norm,
        vec_out[0],
        vec_out[1],
        vec_out[2],
        ada_out[0],
        ada_out[1],
        ada_out[2],
        qkv_out[0],
        qkv_out[1],
        qkv_out[2],
        attn_out[0],
        attn_out[1],
        attn_out[2],
        in_out[0],
        in_out[1],
        in_out[2],
        out_out[0],
        out_out[1],
        out_out[2],
    )


F32, BF = jnp.float32, jnp.bfloat16
MESH = pl.DeviceIdType.MESH
DP, LINE, SEQ, CHIPS, ALL = 4, 4, 8, 16, 32
ROWS, WIDTH, PACK = 128, 768, 640
HALF = WIDTH // 2
HALVES = ((0, 0), (0, 1), (0, 2), (2, 2), (1, 0), (1, 1), (1, 2), None, (2, 0), (2, 1))

def numbered(**counts):
    at = {}
    for name, count in counts.items():
        at[name] = sum(counts[other] for other in at)
    return SimpleNamespace(**at), sum(counts.values())


S, SEM_COUNT = numbered(
    cond=1,
    mix_qkv=1,
    mix_in=1,
    mix_attn=1,
    mod=1,
    w_qkv=1,
    w_in=1,
    w_attn=1,
    w_out=1,
    h1=4,
    h2=4,
    dm=4,
    x=4,
    xf=4,
    o=1,
    mm=1,
    dh2=1,
    do=1,
    gp=1,
    gx=4,
    dh1=1,
    pair_out=1,
    pair_in=1,
    pair_attn=1,
    pair_qkv=1,
    line_out=1,
    line_in=1,
    line_attn=1,
    line_qkv=1,
    last_in=1,
    last_attn=1,
    last_qkv=1,
    early=1,
    early2=1,
    late=1,
    late2=1,
    sq=1,
    fw_qkv=1,
    fw_in=1,
    fw_attn=1,
    fw_out=1,
)

SCRATCH = dict(
    wide_qkv=((48, 3072), F32),
    wide_in=((48, 3072), F32),
    wide_attn=((48, 768), F32),
    s_qkv=((48, 3072), BF),
    s_in=((48, 3072), BF),
    s_attn=((48, 768), BF),
    s_out=((96, 768), BF),
    w_qkv=((768, 768), BF),
    w_in=((768, 768), BF),
    w_attn=((768, 768), BF),
    w_out=((4, 2, 96, 768), BF),
    conds_all=((4, 8, 128), F32),
    mod_send=((4, 4, 128), F32),
    mod_got=((32, 4, 128), F32),
    mod_flat=((40, 128), F32),
    mod=((8, 768), F32),
    x0=((128, 768), F32),
    n1=((128, 768), F32),
    inv1=((128, 128), F32),
    x1=((128, 768), F32),
    n2=((128, 768), F32),
    inv2=((128, 128), F32),
    a=((128, 768), F32),
    dx1=((128, 768), F32),
    h1=((4, 128, 768), BF),
    h2=((4, 128, 768), BF),
    dm=((4, 128, 768), BF),
    gb=((4, 128, 768), BF),
    du=((4, 128, 768), BF),
    xs=((4, 128, 640), BF),
    xb=((2, 4, 128, 640), BF),
    pt=((3, 1024, 512), BF),
    ot=((2, 128, 512), F32),
    os=((4, 128, 256), BF),
    ob=((4, 128, 256), BF),
    mms=((4, 128, 768), BF),
    mmr=((4, 128, 768), BF),
    dhs=((4, 128, 768), BF),
    dhr=((4, 128, 768), BF),
    das=((128, 768), BF),
    dos=((4, 128, 256), BF),
    dob=((4, 128, 256), BF),
    dst=((1024, 512), BF),
    ga=((1024, 640), F32),
    gps=((512, 512), BF),
    gpr=((512, 512), BF),
    gs=((4, 128, 640), BF),
    gx=((4, 128, 640), BF),
    dqkv=((4, 128, 640), BF),
    d1s=((4, 128, 768), BF),
    d1r=((4, 128, 768), BF),
    g_out=((4, 2, 96, 768), BF),
    g_in=((768, 768), BF),
    g_attn=((768, 768), BF),
    g_qkv=((768, 640), BF),
    p_out=((4, 96, 768), BF),
    p_in=((384, 768), BF),
    p_attn=((384, 768), BF),
    p_qkv=((384, 640), BF),
    r_out=((4, 96, 768), BF),
    r_in=((8, 48, 768), BF),
    r_attn=((8, 48, 768), BF),
    r_qkv=((8, 48, 640), BF),
    t_in=((2, 48, 768), F32),
    t_attn=((2, 48, 768), F32),
    t_qkv=((2, 48, 640), F32),
    f_in=((4, 24, 768), F32),
    f_attn=((4, 24, 768), F32),
    f_qkv=((4, 24, 640), F32),
    early=((8, 768), F32),
    early_got=((8, 8, 768), F32),
    early_all=((4, 8, 768), F32),
    late=((4, 768), F32),
    late_got=((8, 4, 768), F32),
    late_all=((4, 4, 768), F32),
    sq=((32, 1, 128), F32),
)


def dot(left, right):
    return jnp.dot(left, right, preferred_element_type=F32)


def dot_nt(left, right):
    return lax.dot_general(left, right, (((1,), (1,)), ((), ())), preferred_element_type=F32)


def dot_tn(left, right):
    return lax.dot_general(left, right, (((0,), (0,)), ((), ())), preferred_element_type=F32)


def loop(count, body, start=0):
    def step(index, carry):
        body(index)
        return carry

    lax.fori_loop(start, count, step, 0)


def layer_kernel(
    i_tok,
    i_cot,
    i_cond,
    i_hide,
    i_vec,
    i_wada,
    i_wqkv,
    i_wattn,
    i_win,
    i_wout,
    i_turn,
    o_y,
    o_dx,
    o_norm,
    o_gqkv,
    o_gattn,
    o_gin,
    o_gout,
    o_dmod,
    o_gvec,
    o_conds,
    *scratch,
):
    r = SimpleNamespace(**dict(zip(SCRATCH, scratch)))
    send_sems, recv_sems = scratch[-2:]
    b, s = lax.axis_index("dp"), lax.axis_index("seq")
    z, c = lax.div(s, 2), lax.rem(s, 2)
    mate = s + 1 - 2 * c
    chip = b * LINE + z
    me = b * SEQ + s
    drains = []

    def push(src, dst, at, to_b, to_s):
        pltpu.make_async_remote_copy(
            src_ref=src,
            dst_ref=dst,
            send_sem=send_sems.at[at],
            recv_sem=recv_sems.at[at],
            device_id=(to_b, to_s),
            device_id_type=MESH,
        ).start()

    def keep(src, dst, at):
        pltpu.make_async_copy(src, dst, recv_sems.at[at]).start()

    def got(at, like):
        pltpu.make_async_copy(like, like, recv_sems.at[at]).wait()

    def left(at, like):
        pltpu.make_async_copy(like, like, send_sems.at[at]).wait()

    def sent(at, like):
        drains.append((at, like))

    def peers(body):
        for k in (1, 2, 3):
            body(lax.rem(b + k, DP))

    def stack(body):
        for k in (1, 2, 3):
            body(lax.rem(z + k, LINE))

    lane = lax.broadcasted_iota(jnp.int32, (1, 128), 1)
    low = lane < 64
    own24 = pl.ds(pl.multiple_of(24 * c, 8), 24)
    mate24 = pl.ds(pl.multiple_of(24 * (1 - c), 8), 24)
    part = pl.ds(pl.multiple_of(HALF * c, 128), HALF)
    chip_rows = pl.ds(pl.multiple_of(48 * chip, 16), 48)

    barrier = pltpu.get_barrier_semaphore()

    def greet(k):
        other = lax.rem(me + k, ALL)
        pl.semaphore_signal(
            barrier, inc=1, device_id=(lax.div(other, SEQ), lax.rem(other, SEQ)), device_id_type=MESH
        )

    loop(ALL, greet, 1)

    def natural(kind, p, head):
        return kind * WIDTH + 192 * p + 64 * head

    def half_at(ref, column, high):
        tile = ref[:, column // 128 * 128 : column // 128 * 128 + 128]
        return tile if (column % 128 == 64) == high else pltpu.roll(tile, 64, 1)

    for p in range(4):
        for tile in range(5):
            pair = []
            for high in (0, 1):
                which = HALVES[2 * tile + high]
                pair.append(
                    jnp.zeros((24, 128), F32)
                    if which is None
                    else half_at(i_wqkv, natural(which[0], p, which[1]), bool(high))
                )
            r.wide_qkv[own24, 768 * p + 128 * tile : 768 * p + 128 * tile + 128] = jnp.where(
                low, pair[0], pair[1]
            )
        r.wide_qkv[own24, 768 * p + 640 : 768 * p + 768] = jnp.zeros((24, 128), F32)
    r.wide_in[own24, :] = i_win[...]
    r.wide_attn[own24, :] = i_wattn[...]
    r.s_out[...] = i_wout[...].astype(BF)
    r.conds_all[b] = i_cond[...]
    pl.semaphore_wait(barrier, ALL - 1)

    peers(lambda to: push(r.conds_all.at[b], r.conds_all.at[b], S.cond, to, s))
    sent(S.cond, r.conds_all.at[0:3])
    push(r.wide_qkv.at[own24], r.wide_qkv.at[own24], S.mix_qkv, b, mate)
    sent(S.mix_qkv, r.wide_qkv.at[0:24])
    push(r.wide_attn.at[own24], r.wide_attn.at[own24], S.mix_attn, b, mate)
    sent(S.mix_attn, r.wide_attn.at[0:24])
    push(r.wide_in.at[own24], r.wide_in.at[own24], S.mix_in, b, mate)
    sent(S.mix_in, r.wide_in.at[0:24])

    got(S.cond, r.conds_all.at[0:3])
    row8 = lax.broadcasted_iota(jnp.int32, (8, 128), 0)
    cond4 = jnp.zeros((8, 128), F32)
    for k in range(4):
        cond4 = jnp.where(row8 == k, r.conds_all[k], cond4)
    o_conds[...] = cond4
    columns = dot(cond4.astype(BF), i_wada[...])
    columns = pltpu.roll(columns, lax.rem(144 * me, 128), 1)
    for k in range(4):
        for t in range(3):
            r.mod_send[k, t : t + 1, :] = columns[k : k + 1, 128 * t : 128 * t + 128]
        r.mod_send[k, 3:4, :] = jnp.zeros((1, 128), F32)

    def send_mod(k):
        other = lax.rem(me + k, ALL)
        ob = lax.div(other, SEQ)
        push(r.mod_send.at[ob], r.mod_got.at[me], S.mod, ob, lax.rem(other, SEQ))

    loop(ALL, send_mod, 1)
    sent(S.mod, r.mod_got.at[0:31])
    keep(r.mod_send.at[b], r.mod_got.at[me], S.mod)

    def spread(src, dst, name, sliced):
        def one(k):
            to = lax.rem(chip + k, CHIPS)
            to_b, to_z = lax.div(to, LINE), lax.rem(to, LINE)
            first = WIDTH * to_b + HALF * c if sliced else HALF * c
            push(
                src.at[:, pl.ds(pl.multiple_of(first, 128), HALF)],
                dst.at[chip_rows, part],
                name,
                to_b,
                2 * to_z + c,
            )

        loop(CHIPS, one, 1)
        first = WIDTH * b + HALF * c if sliced else HALF * c
        keep(src.at[:, pl.ds(pl.multiple_of(first, 128), HALF)], dst.at[chip_rows, part], name)
        sent(name, dst.at[0:720, 0:HALF])

    def share(dst, name, onward):
        got(name, dst.at[:, part])
        push(dst.at[:, part], dst.at[:, part], onward, b, mate)
        sent(onward, dst.at[:, 0:HALF])

    got(S.mix_qkv, r.wide_qkv.at[0:24])
    r.s_qkv[...] = r.wide_qkv[...].astype(BF)
    spread(r.s_qkv, r.w_qkv, S.w_qkv, True)
    got(S.mix_attn, r.wide_attn.at[0:24])
    r.s_attn[...] = r.wide_attn[...].astype(BF)
    got(S.mix_in, r.wide_in.at[0:24])
    r.s_in[...] = r.wide_in[...].astype(BF)

    got(S.mod, r.mod_got)
    r.mod_flat[...] = jnp.zeros((40, 128), F32)
    for k in range(ALL):
        first = 9 * k // 8
        r.mod_flat[first : first + 3, :] += r.mod_got[k, 0:3, :]
    for k in range(6):
        row = jnp.concatenate(
            [r.mod_flat[6 * k + t : 6 * k + t + 1, :] for t in range(6)], axis=1
        )
        r.mod[k : k + 1, :] = row + i_vec[2 + k : 3 + k, :]

    def mod(k):
        return r.mod[k : k + 1, :]

    def vec(k):
        return i_vec[k : k + 1, :]

    hidden = i_hide[:, 0:1] > 0.5

    x0 = jnp.where(hidden, vec(8), i_tok[...].astype(F32))
    r.x0[...] = x0
    n1, inv1 = normalize(x0)
    r.n1[...] = n1
    r.inv1[...] = jnp.broadcast_to(inv1, (ROWS, 128))
    r.h1[b] = (n1 * vec(0) * (1.0 + mod(1)) + mod(0)).astype(BF)
    peers(lambda to: push(r.h1.at[b], r.h1.at[b], S.h1 + b, to, s))
    sent(S.h1 + b, r.h1.at[0:3])
    r.dm[b] = (i_cot[...].astype(F32) * mod(5)).astype(BF)
    spread(r.s_attn, r.w_attn, S.w_attn, False)

    share(r.w_qkv, S.w_qkv, S.fw_qkv)
    peers(lambda to: push(r.dm.at[b], r.dm.at[b], S.dm + b, to, s))
    sent(S.dm + b, r.dm.at[0:3])
    got(S.fw_qkv, r.w_qkv.at[:, 0:HALF])
    cosines, back_sines, fore_sines = i_turn[0], i_turn[1], i_turn[2]

    def turned(tile, sign):
        return (
            tile * cosines
            + sign * (pltpu.roll(tile, 96, 1) * back_sines + pltpu.roll(tile, 32, 1) * fore_sines)
        )

    def project(j):
        to = lax.rem(z + 1 + j, LINE)

        @pl.when(to != b)
        def _():
            got(S.h1 + to, r.h1.at[0])

        x = dot(r.h1[to], r.w_qkv[:, 0:PACK])
        tiles = [x[:, 128 * t : 128 * t + 128] for t in range(5)]
        tiles[0] = turned(tiles[0], 1.0) * 0.125
        tiles[1] = jnp.where(low, turned(tiles[1], 1.0) * 0.125, tiles[1])
        tiles[2] = turned(tiles[2], 1.0)
        tiles[3] = turned(tiles[3], 1.0)
        for t in range(5):
            r.xs[to, :, 128 * t : 128 * t + 128] = tiles[t].astype(BF)

        @pl.when(j < 3)
        def _():
            push(r.xs.at[to], r.xb.at[0, z], S.x + z, b, 2 * to + c)

        @pl.when(j == 3)
        def _():
            keep(r.xs.at[to], r.xb.at[0, z], S.x + z)

    loop(4, project)
    sent(S.x + z, r.xs.at[0:3])

    def pass_on(k):
        source = lax.rem(z + k, LINE)
        got(S.x + source, r.xs.at[0])
        push(r.xb.at[0, source], r.xb.at[1, source], S.xf + source, b, mate)

    loop(4, pass_on)
    for k in range(4):
        sent(S.xf + k, r.xs.at[0])

    def send_out(to):
        push(r.s_out, r.w_out.at[z, c], S.w_out, b, 2 * to + c)

    stack(send_out)
    keep(r.s_out, r.w_out.at[z, c], S.w_out)
    sent(S.w_out, r.w_out.at[0:3, 0])
    spread(r.s_in, r.w_in, S.w_in, True)
    for k in range(4):
        got(S.xf + k, r.xs.at[0])

    def tile_of(t):
        return r.xb[:, :, :, 128 * t : 128 * t + 128].reshape(1024, 128)

    heads = ((0, 2, 4, True, True), (0, 2, 4, False, False), (1, 3, 1, True, False))

    def queries(head, first, size):
        q_tile, _, _, q_low, _ = heads[head]
        q = r.xb[0, first : first + size, :, 128 * q_tile : 128 * q_tile + 128]
        return jnp.where(low if q_low else ~low, q.reshape(size * 128, 128), jnp.zeros((), BF))

    for head in range(3):
        keys, values = tile_of(heads[head][1]), tile_of(heads[head][2])
        for half in range(2):
            at = slice(256 * half, 256 * half + 256)
            scores = dot_nt(keys, queries(head, 2 * half, 2))
            weights = jnp.exp(scores - jnp.max(scores, axis=0, keepdims=True))
            weights = weights * (1.0 / jnp.sum(weights, axis=0, keepdims=True))
            weights = weights.astype(BF)
            r.pt[head, :, at] = weights
            out = dot_tn(values, weights)
            if head == 0:
                r.ot[0, 0:64, at] = out[0:64]
            elif head == 1:
                r.ot[0, 64:128, at] = out[64:128]
            else:
                r.ot[1, 0:64, at] = out[64:128]
                r.ot[1, 64:128, at] = jnp.zeros((64, 256), F32)
    for t in range(2):
        r.os[:, :, 128 * t : 128 * t + 128] = (
            r.ot[t].T.astype(BF).reshape(4, 128, 128)
        )

    def send_o(to):
        push(r.os.at[to], r.ob.at[b], S.o, z, 2 * to + c)

    stack(send_o)

    @pl.when(b == z)
    def _():
        keep(r.os.at[z], r.ob.at[b], S.o)

    @pl.when(b != z)
    def _():
        send_o(z)

    share(r.w_attn, S.w_attn, S.fw_attn)
    got(S.fw_attn, r.w_attn.at[:, 0:HALF])
    got(S.o, r.ob)
    a = jnp.zeros((ROWS, WIDTH), F32)
    for p in range(4):
        a += dot(r.ob[p, :, 0:128], r.w_attn[192 * p : 192 * p + 128, :])
        a += dot(r.ob[p, :, 128:192], r.w_attn[192 * p + 128 : 192 * p + 192, :])
    r.a[...] = a
    x1 = r.x0[...] + mod(2) * a
    r.x1[...] = x1
    n2, inv2 = normalize(x1)
    r.n2[...] = n2
    r.inv2[...] = jnp.broadcast_to(inv2, (ROWS, 128))
    r.h2[b] = (n2 * vec(1) * (1.0 + mod(4)) + mod(3)).astype(BF)
    peers(lambda to: push(r.h2.at[b], r.h2.at[b], S.h2 + b, to, s))
    sent(S.h2 + b, r.h2.at[0:3])
    got(S.w_out, r.w_out.at[:, 0])
    push(r.w_out.at[:, c], r.w_out.at[:, c], S.fw_out, b, mate)
    sent(S.fw_out, r.w_out.at[:, 0])
    share(r.w_in, S.w_in, S.fw_in)
    got(S.fw_out, r.w_out.at[:, 0])
    got(S.fw_in, r.w_in.at[:, 0:HALF])

    def feed(j):
        k = lax.rem(b + j, DP)

        @pl.when(j > 0)
        def _():
            got(S.h2 + k, r.h2.at[0])
            got(S.dm + k, r.dm.at[0])

        u = dot(r.h2[k], r.w_in[...])
        slope = 0.7978845608028654
        cube = 0.044715
        t = jnp.tanh(slope * (u + cube * u * u * u))
        r.gb[k] = (0.5 * u * (1.0 + t)).astype(BF)
        bend = 0.5 * (1.0 + t) + 0.5 * u * (1.0 - t * t) * (slope * (1.0 + 3.0 * cube * u * u))
        r.du[k] = (dot_nt(r.dm[k], r.w_out[...].reshape(768, 768)) * bend).astype(BF)
        r.dhs[k] = dot_nt(r.du[k], r.w_in[...]).astype(BF)

        @pl.when(j > 0)
        def _():
            push(r.dhs.at[k], r.dhr.at[b], S.dh2, k, s)

    loop(4, feed)
    sent(S.dh2, r.dhs.at[0:3])

    def feed_out(j):
        k = lax.rem(b + j, DP)
        r.mms[k] = dot(r.gb[k], r.w_out[...].reshape(768, 768)).astype(BF)

        @pl.when(j > 0)
        def _():
            push(r.mms.at[k], r.mmr.at[b], S.mm, k, s)

    loop(4, feed_out)
    sent(S.mm, r.mms.at[0:3])

    def gather(own, others):
        total = own[b].astype(F32)
        for k in (1, 2, 3):
            total += others[lax.rem(b + k, DP)].astype(F32)
        return total

    for k in range(4):
        rows = slice(192 * k, 192 * k + 192)
        block = dot_tn(r.gb[:, :, rows].reshape(512, 192), r.dm[...].reshape(512, 768))
        r.g_out[k] = block.astype(BF).reshape(2, 96, 768)
    push(r.g_out.at[:, 1 - c], r.p_out, S.pair_out, b, mate)
    sent(S.pair_out, r.p_out)

    def outer(left, right, dst, width):
        def one(k):
            rows = pl.ds(pl.multiple_of(128 * k, 128), 128)
            dst[rows, :] = dot_tn(
                left[:, :, rows].reshape(512, 128), right[...].reshape(512, width)
            ).astype(BF)

        loop(6, one)

    half_rows = pl.ds(pl.multiple_of(HALF * c, 16), HALF)
    mate_rows = pl.ds(pl.multiple_of(HALF * (1 - c), 16), HALF)

    def to_mate(grad, dst, name):
        push(grad.at[mate_rows], dst, name, b, mate)
        sent(name, dst)

    def to_line(grad, pair, dst, first, name):
        got(first, pair)
        grad[half_rows, :] = (grad[half_rows, :].astype(F32) + pair[...].astype(F32)).astype(BF)
        side = lax.rem(b, 2)
        slot = lax.div(b, 2) * 4 + z

        def one(k):
            to_b, to_z = 2 * c + lax.div(k, 4), lax.rem(k, 4)
            src = grad.at[pl.ds(pl.multiple_of(HALF * c + 48 * k, 16), 48)]
            here = (to_b == b) & (to_z == z) & (side == c)

            @pl.when(here)
            def _():
                keep(src, dst.at[slot], name)

            @pl.when(jnp.logical_not(here))
            def _():
                push(src, dst.at[slot], name, to_b, 2 * to_z + side)

        loop(8, one)

    def line_sent(dst, name):
        mine = (lax.div(b, 2) == c) & (lax.rem(b, 2) == c)

        @pl.when(mine)
        def _():
            left(name, dst.at[0:7])

        @pl.when(jnp.logical_not(mine))
        def _():
            left(name, dst)

    def last_mix(dst, total, final, name, onward):
        got(name, dst)
        for k in range(2):
            total[k] = (dst[4 * k].astype(F32) + dst[4 * k + 1].astype(F32)) + (
                dst[4 * k + 2].astype(F32) + dst[4 * k + 3].astype(F32)
            )
            push(total.at[k, mate24], final.at[2 * k + c], onward, b, mate)
            final[2 * k + c] = total[k, own24, :]
        sent(onward, final.at[0:2])

    outer(r.h2, r.du, r.g_in, 768)
    to_mate(r.g_in, r.p_in, S.pair_in)

    got(S.dh2, r.dhr.at[0:3])
    dh = gather(r.dhs, r.dhr)
    n2 = r.n2[...]
    inv2 = r.inv2[:, 0:1]
    r.early[...] = jnp.zeros((8, 768), F32)
    r.early[2:3, :] = jnp.sum(dh, axis=0, keepdims=True)
    both = jnp.sum(dh * n2, axis=0, keepdims=True)
    r.early[3:4, :] = both * vec(1)
    r.early[0:1, :] = both * (1.0 + mod(4))
    grad = dh * ((1.0 + mod(4)) * vec(1))
    dx1 = i_cot[...].astype(F32) + norm_back(n2, inv2, grad)
    r.dx1[...] = dx1
    r.early[1:2, :] = jnp.sum(dx1 * r.a[...], axis=0, keepdims=True)
    r.das[...] = (dx1 * mod(2)).astype(BF)
    for p in range(4):
        first = 192 * p
        r.dos[p, :, 0:128] = dot_nt(r.das[...], r.w_attn[first : first + 128, :]).astype(BF)
        tail = dot_nt(r.das[...], r.w_attn[first + 128 : first + 192, :])
        r.dos[p, :, 128:256] = jnp.concatenate(
            [tail, jnp.zeros((ROWS, 64), F32)], axis=1
        ).astype(BF)

    def send_do(to):
        push(r.dos.at[to], r.dob.at[z], S.do, to, 2 * b + c)

    peers(send_do)

    @pl.when(b == z)
    def _():
        keep(r.dos.at[b], r.dob.at[z], S.do)

    @pl.when(b != z)
    def _():
        send_do(b)

    for p in range(4):
        rows = slice(192 * p, 192 * p + 192)
        r.g_attn[rows, :] = dot_tn(r.ob[p], r.das[...])[0:192].astype(BF)
    to_mate(r.g_attn, r.p_attn, S.pair_attn)

    got(S.mm, r.mmr.at[0:3])
    mm = gather(r.mms, r.mmr)
    o_y[...] = r.x1[...] + mod(5) * mm
    r.early[4:5, :] = jnp.sum(i_cot[...].astype(F32) * mm, axis=0, keepdims=True)

    def over_line(src, dst, name):
        def one(k):
            push(src, dst.at[s], name, b, lax.rem(s + k, SEQ))

        loop(SEQ, one, 1)
        keep(src, dst.at[s], name)
        sent(name, dst.at[0:7])

    def over_group(got_ref, dst, name):
        total = got_ref[0]
        for k in range(1, SEQ):
            total += got_ref[k]
        dst[b] = total
        peers(lambda to: push(dst.at[b], dst.at[b], name, to, s))
        sent(name, dst.at[0:3])

    over_line(r.early, r.early_got, S.early)

    got(S.pair_out, r.p_out)
    for k in range(4):
        r.g_out[k, c] = (r.g_out[k, c].astype(F32) + r.p_out[k].astype(F32)).astype(BF)

    def send_gout(to):
        push(r.g_out.at[to, c], r.r_out.at[z], S.line_out, b, 2 * to + c)

    stack(send_gout)
    keep(r.g_out.at[z, c], r.r_out.at[z], S.line_out)
    sent(S.line_out, r.r_out.at[0:3])
    to_line(r.g_in, r.p_in, r.r_in, S.pair_in, S.line_in)

    got(S.do, r.dob)
    dot0, dot1 = r.dob[:, :, 0:128].reshape(512, 128), r.dob[:, :, 128:256].reshape(512, 128)
    zero = jnp.zeros((), BF)
    moved = pltpu.roll(dot1.astype(F32), 64, 1).astype(BF)
    grads = (jnp.where(low, dot0, zero), jnp.where(low, zero, dot0), moved)
    product = dot0.astype(F32).T * r.ot[0]
    deltas = (
        jnp.sum(product[0:64], axis=0, keepdims=True),
        jnp.sum(product[64:128], axis=0, keepdims=True),
        jnp.sum(dot1.astype(F32).T * r.ot[1], axis=0, keepdims=True),
    )
    turned_q = []
    for head in range(3):
        keys, values = tile_of(heads[head][1]), tile_of(heads[head][2])
        for half in range(2):
            at = slice(256 * half, 256 * half + 256)
            dp = dot_nt(values, grads[head][at])
            ds = (r.pt[head, :, at].astype(F32) * (dp - deltas[head][:, at])).astype(BF)
            r.dst[:, at] = ds
            turned_q.append(dot_tn(keys, ds))
        dk = dot(r.dst[...], queries(head, 0, 4))
        dv = dot(r.pt[head], grads[head])
        if head == 0:
            r.ga[:, 256:384] = dk
            r.ga[:, 512:640] = dv
        elif head == 1:
            r.ga[:, 256:384] += dk
            r.ga[:, 512:640] += dv
        else:
            r.ga[:, 384:512] = dk
            r.ga[:, 128:256] = dv
    r.gps[...] = r.ga[512:1024, 128:640].astype(BF)
    push(r.gps, r.gpr, S.gp, b, mate)
    sent(S.gp, r.gps)
    for half in range(2):
        at = slice(256 * half, 256 * half + 256)
        top = jnp.concatenate([turned_q[half][0:64], turned_q[2 + half][64:128]], axis=0)
        r.ga[at, 0:128] = top.T * 0.125
        r.ga[at, 128:256] += turned_q[4 + half].T * 0.125
    got(S.gp, r.gpr)
    r.gs[:, :, 0:128] = r.ga[0:512, 0:128].astype(BF).reshape(4, 128, 128)
    r.gs[:, :, 128:640] = (
        (r.ga[0:512, 128:640] + r.gpr[...].astype(F32)).astype(BF).reshape(4, 128, 512)
    )

    def send_g(to):
        push(r.gs.at[to], r.gx.at[z], S.gx + z, b, 2 * to + c)

    stack(send_g)
    keep(r.gs.at[z], r.gx.at[z], S.gx + z)
    sent(S.gx + z, r.gs.at[0:3])
    to_line(r.g_attn, r.p_attn, r.r_attn, S.pair_attn, S.line_attn)
    got(S.early, r.early_got)
    over_group(r.early_got, r.early_all, S.early2)

    def unproject(j):
        k = lax.rem(z + j, LINE)
        got(S.gx + k, r.gx.at[0])
        g = r.gx[k].astype(F32)
        tiles = [g[:, 128 * t : 128 * t + 128] for t in range(5)]
        tiles[0] = turned(tiles[0], -1.0)
        tiles[1] = jnp.where(low, turned(tiles[1], -1.0), tiles[1])
        tiles[2] = turned(tiles[2], -1.0)
        tiles[3] = turned(tiles[3], -1.0)
        for t in range(5):
            r.dqkv[k, :, 128 * t : 128 * t + 128] = tiles[t].astype(BF)
        r.d1s[k] = dot_nt(r.dqkv[k], r.w_qkv[:, 0:PACK]).astype(BF)

        @pl.when(k != b)
        def _():
            push(r.d1s.at[k], r.d1r.at[b], S.dh1, k, s)

    loop(4, unproject)
    sent(S.dh1, r.d1s.at[0:3])
    outer(r.h1, r.dqkv, r.g_qkv, 640)
    to_mate(r.g_qkv, r.p_qkv, S.pair_qkv)
    last_mix(r.r_in, r.t_in, r.f_in, S.line_in, S.last_in)
    to_line(r.g_qkv, r.p_qkv, r.r_qkv, S.pair_qkv, S.line_qkv)

    got(S.dh1, r.d1r.at[0:3])
    dh = gather(r.d1s, r.d1r)
    n1 = r.n1[...]
    both = jnp.sum(dh * n1, axis=0, keepdims=True)
    r.late[0:1, :] = both * (1.0 + mod(1))
    r.late[1:2, :] = jnp.sum(dh, axis=0, keepdims=True)
    r.late[2:3, :] = both * vec(0)
    grad = dh * ((1.0 + mod(1)) * vec(0))
    dx0 = r.dx1[...] + norm_back(n1, r.inv1[:, 0:1], grad)
    o_dx[...] = dx0
    r.late[3:4, :] = jnp.sum(jnp.where(hidden, dx0, 0.0), axis=0, keepdims=True)
    over_line(r.late, r.late_got, S.late)

    got(S.line_out, r.r_out)
    total = (r.r_out[0].astype(F32) + r.r_out[1].astype(F32)) + (
        r.r_out[2].astype(F32) + r.r_out[3].astype(F32)
    )
    o_gout[...] = total
    squares = total * total
    squares = jnp.sum(squares[:, 0:128] + squares[:, 128:256] + squares[:, 256:384]
                      + squares[:, 384:512] + squares[:, 512:640] + squares[:, 640:768],
                      axis=0, keepdims=True)

    def fold(value):
        total = value[:, 0:128] * value[:, 0:128]
        for t in range(1, value.shape[1] // 128):
            total += value[:, 128 * t : 128 * t + 128] * value[:, 128 * t : 128 * t + 128]
        return jnp.sum(total, axis=0, keepdims=True)

    last_mix(r.r_attn, r.t_attn, r.f_attn, S.line_attn, S.last_attn)
    got(S.late, r.late_got)
    over_group(r.late_got, r.late_all, S.late2)
    got(S.last_in, r.f_in.at[0:2])
    for p in range(4):
        value = r.f_in[p]
        o_gin[:, 768 * p : 768 * p + 768] = value
        squares += fold(value)
    got(S.last_attn, r.f_attn.at[0:2])
    value = (r.f_attn[0] + r.f_attn[1]) + (r.f_attn[2] + r.f_attn[3])
    o_gattn[...] = value
    squares += fold(value)
    last_mix(r.r_qkv, r.t_qkv, r.f_qkv, S.line_qkv, S.last_qkv)
    got(S.last_qkv, r.f_qkv.at[0:2])
    where = {which: index for index, which in enumerate(HALVES) if which is not None}

    def packed_half(chunk, high):
        kind, rest = chunk // 12, chunk % 12
        index = where[(kind, rest % 3)]
        tile = r.f_qkv[rest // 3, :, index // 2 * 128 : index // 2 * 128 + 128]
        return tile if index % 2 == high else pltpu.roll(tile, 64, 1)

    for t in range(18):
        o_gqkv[:, 128 * t : 128 * t + 128] = jnp.where(
            low, packed_half(2 * t, 0), packed_half(2 * t + 1, 1)
        )
    for p in range(4):
        squares += fold(r.f_qkv[p])

    r.sq[me] = squares

    def send_sq(k):
        other = lax.rem(me + k, ALL)
        push(r.sq.at[me], r.sq.at[me], S.sq, lax.div(other, SEQ), lax.rem(other, SEQ))

    loop(ALL, send_sq, 1)
    sent(S.sq, r.sq.at[0:31])
    got(S.early2, r.early_all.at[0:3])
    got(S.late2, r.late_all.at[0:3])
    mods = []
    for k in range(4):
        early, late = r.early_all[k], r.late_all[k]
        rows = jnp.concatenate([late[1:3], early[1:5], jnp.zeros((2, 768), F32)], axis=0)
        o_dmod[k] = rows
        mods.append(rows)
    gain = jnp.concatenate(
        [
            sum(r.late_all[k][0:1] for k in range(4)),
            sum(r.early_all[k][0:1] for k in range(4)),
            (mods[0] + mods[1] + mods[2] + mods[3])[0:6],
        ],
        axis=0,
    )
    mask_row = sum(r.late_all[k][3:4] for k in range(4))
    o_gvec[0:8, :] = gain
    o_gvec[8:9, :] = mask_row
    o_gvec[9:16, :] = jnp.zeros((7, 768), F32)
    small = jnp.sum(gain * gain) + jnp.sum(mask_row * mask_row)
    conds = [r.conds_all[k][0:1].astype(BF).astype(F32) for k in range(4)]
    for k in range(4):
        for m in range(k, 4):
            term = jnp.sum(mods[k] * mods[m]) * jnp.sum(conds[k] * conds[m])
            small += term if m == k else 2.0 * term
    got(S.sq, r.sq.at[0:31])
    total = r.sq[0]
    for k in range(1, ALL):
        total += r.sq[k]
    o_norm[...] = jnp.broadcast_to(jnp.sqrt(jnp.sum(total) + small), (8, 128))

    for at, like in drains:
        left(at, like)
    for name, dst in ((S.line_in, r.r_in), (S.line_attn, r.r_attn), (S.line_qkv, r.r_qkv)):
        line_sent(dst, name)
    for name, like in ((S.o, r.os), (S.do, r.dos)):

        @pl.when(b == z)
        def _():
            left(name, like.at[0:3])

        @pl.when(b != z)
        def _():
            left(name, like)


def run_layer(*args):
    shapes = (
        ((ROWS, WIDTH), F32),
        ((ROWS, WIDTH), F32),
        ((8, 128), F32),
        ((24, 3 * WIDTH), F32),
        ((24, WIDTH), F32),
        ((24, 4 * WIDTH), F32),
        ((96, WIDTH), F32),
        ((4, 8, WIDTH), F32),
        ((16, WIDTH), F32),
        ((8, 128), F32),
    )
    whole = pl.BlockSpec(memory_space=pltpu.VMEM)
    return pl.pallas_call(
        layer_kernel,
        out_shape=[jax.ShapeDtypeStruct(shape, kind) for shape, kind in shapes],
        in_specs=[whole] * len(args),
        out_specs=[whole] * len(shapes),
        scratch_shapes=[pltpu.VMEM(shape, kind) for shape, kind in SCRATCH.values()]
        + [pltpu.SemaphoreType.DMA((SEM_COUNT,)), pltpu.SemaphoreType.DMA((SEM_COUNT,))],
        compiler_params=pltpu.CompilerParams(
            collective_id=0, has_side_effects=True, vmem_limit_bytes=60 * 1024 * 1024
        ),
    )(*args)


def slices(
    tokens_in,
    cotangent,
    timesteps,
    span_start,
    span_len,
    vectors,
    w_ada,
    w_qkv,
    w_attn,
    w_in,
    w_out,
    m_vec,
    v_vec,
    m_ada,
    v_ada,
    m_qkv,
    v_qkv,
    m_attn,
    v_attn,
    m_in,
    v_in,
    m_out,
    v_out,
):
    positions = lax.axis_index("seq") * ROWS + jnp.arange(ROWS, dtype=jnp.int32)
    masked = (positions >= span_start[0]) & (positions < span_start[0] + span_len[0])
    masked = masked[:, None]
    cosines, sines = rotary_tables(positions)
    none = jnp.zeros_like(sines)
    turn = jnp.stack(
        [
            jnp.concatenate([cosines] * 4, axis=1),
            jnp.concatenate([-sines, none] * 2, axis=1),
            jnp.concatenate([none, sines] * 2, axis=1),
        ]
    )
    cond = jnp.broadcast_to(cond_input(timesteps), (8, COND))
    y, dx0, norm, g_qkv, g_attn, g_in, g_out, dmod, g_vec, conds = run_layer(
        tokens_in[0],
        cotangent[0],
        cond,
        jnp.broadcast_to(masked.astype(F32), (ROWS, 128)),
        vectors,
        jnp.pad(w_ada.astype(BF), ((0, 0), (0, 384 - w_ada.shape[1]))),
        w_qkv,
        w_attn,
        w_in,
        w_out,
        turn,
    )
    block_out = y.astype(BF)[None]
    grad_input = jnp.where(masked, 0.0, dx0)[None]
    grad_norm = norm[0, 0]
    clip_factor = jnp.minimum(1.0, CLIP / (grad_norm + 1e-06))
    rank = lax.axis_index(("dp", "seq"))
    wide, narrow = w_ada.shape[1], m_vec.shape[1]
    own_mod = lax.dynamic_slice_in_dim(
        dmod[:, 0:6].reshape(4, 6 * WIDTH), rank * wide, wide, 1
    )
    g_ada = jnp.dot(
        conds[0:4].astype(BF).astype(F32).T, own_mod, precision=lax.Precision.HIGHEST
    )
    g_vec = lax.dynamic_slice_in_dim(g_vec[0:9], rank * narrow, narrow, 1)
    own_vectors = lax.dynamic_slice_in_dim(vectors, rank * narrow, narrow, 1)
    vec_out = adam_step(own_vectors, g_vec * clip_factor, m_vec, v_vec, RATE_VECTORS, 0.0)
    ada_out = adam_step(w_ada, g_ada * clip_factor, m_ada, v_ada, RATE, DECAY)
    qkv_out = adam_step(w_qkv, g_qkv * clip_factor, m_qkv, v_qkv, RATE, DECAY)
    attn_out = adam_step(w_attn, g_attn * clip_factor, m_attn, v_attn, RATE, DECAY)
    in_out = adam_step(w_in, g_in * clip_factor, m_in, v_in, RATE, DECAY)
    out_out = adam_step(w_out, g_out * clip_factor, m_out, v_out, RATE, DECAY)
    return (
        block_out,
        grad_input,
        grad_norm,
        *vec_out,
        *ada_out,
        *qkv_out,
        *attn_out,
        *in_out,
        *out_out,
    )


def solution(mesh):
    in_specs = (
        P("dp", "seq", None),
        P("dp", "seq", None),
        P("dp"),
        P("dp"),
        P("dp"),
        P(),
        P(None, ("dp", "seq")),
        P(("dp", "seq"), None),
        P(("dp", "seq"), None),
        P(("dp", "seq"), None),
        P(("dp", "seq"), None),
        P(None, ("dp", "seq")),
        P(None, ("dp", "seq")),
        P(None, ("dp", "seq")),
        P(None, ("dp", "seq")),
        P(("dp", "seq"), None),
        P(("dp", "seq"), None),
        P(("dp", "seq"), None),
        P(("dp", "seq"), None),
        P(("dp", "seq"), None),
        P(("dp", "seq"), None),
        P(("dp", "seq"), None),
        P(("dp", "seq"), None),
    )
    out_specs = (
        P("dp", "seq", None),
        P("dp", "seq", None),
        P(),
        P(None, ("dp", "seq")),
        P(None, ("dp", "seq")),
        P(None, ("dp", "seq")),
        P(None, ("dp", "seq")),
        P(None, ("dp", "seq")),
        P(None, ("dp", "seq")),
        P(("dp", "seq"), None),
        P(("dp", "seq"), None),
        P(("dp", "seq"), None),
        P(("dp", "seq"), None),
        P(("dp", "seq"), None),
        P(("dp", "seq"), None),
        P(("dp", "seq"), None),
        P(("dp", "seq"), None),
        P(("dp", "seq"), None),
        P(("dp", "seq"), None),
        P(("dp", "seq"), None),
        P(("dp", "seq"), None),
    )
    sizes = dict(mesh.shape)
    local = slices if (sizes["dp"], sizes["seq"]) == (4, 8) else plain
    return jax.shard_map(local, mesh=mesh, in_specs=in_specs, out_specs=out_specs, check_vma=False)
```

```python
from functools import partial
import math
from types import SimpleNamespace

import jax
import jax.numpy as jnp
from jax import lax
from jax.experimental import pallas as pl
from jax.experimental.pallas import tpu as pltpu
from jax.sharding import PartitionSpec as P

HD = 64
COND = 128
STEP = 10


BETA_ONE = 0.9
BETA_TWO = 0.999
ADAM_EPS = 1e-08
RATE = 0.1
RATE_VECTORS = 0.3
DECAY = 0.01
CLIP = 1.0
NORM_EPS = 1e-05


def cond_input(timesteps):
    half_cond = COND // 2
    freqs = jnp.exp(jnp.arange(half_cond, dtype=jnp.float32) * (-math.log(10000.0) / half_cond))
    angles = timesteps.astype(jnp.float32)[:, None] * freqs[None, :]
    return jax.nn.silu(jnp.concatenate([jnp.cos(angles), jnp.sin(angles)], axis=1))


def rotary_tables(positions):
    half_head = HD // 2
    inverse = jnp.exp(jnp.arange(half_head, dtype=jnp.float32) * (-math.log(10000.0) / half_head))
    angles = positions.astype(jnp.float32)[:, None] * inverse[None, :]
    return (jnp.cos(angles), jnp.sin(angles))


def rotate(values, cosines, sines):
    half_head = values.shape[-1] // 2
    first = values[..., :half_head]
    second = values[..., half_head:]
    cos_b = cosines[:, None, :]
    sin_b = sines[:, None, :]
    return jnp.concatenate(
        [first * cos_b - second * sin_b, second * cos_b + first * sin_b], axis=-1
    )


def rotate_back(grads, cosines, sines):
    half_head = grads.shape[-1] // 2
    first = grads[..., :half_head]
    second = grads[..., half_head:]
    cos_b = cosines[:, None, :]
    sin_b = sines[:, None, :]
    return jnp.concatenate(
        [first * cos_b + second * sin_b, second * cos_b - first * sin_b], axis=-1
    )


def normalize(values):
    centre = jnp.mean(values, axis=-1, keepdims=True)
    centred = values - centre
    inverse = lax.rsqrt(jnp.mean(centred * centred, axis=-1, keepdims=True) + NORM_EPS)
    return (centred * inverse, inverse)


def norm_back(normed, inverse, grad):
    return inverse * (
        grad
        - jnp.mean(grad, axis=-1, keepdims=True)
        - normed * jnp.mean(grad * normed, axis=-1, keepdims=True)
    )


def split_kv(block, width):
    seqs, block_rows = (block.shape[0], block.shape[1])
    keys = block[..., :width].reshape(seqs, block_rows, width // HD, HD)
    values = block[..., width:].reshape(seqs, block_rows, width // HD, HD)
    return (keys, values)


def attend_piece(carry, piece, queries, width, factor):
    piece_rows = piece.shape[1]
    size = math.gcd(piece_rows, 512)

    def attend_one_block(index, state):
        running, denom, accum = state
        block = lax.dynamic_slice_in_dim(piece, index * size, size, 1)
        keys, values = split_kv(block, width)
        scores = (
            jnp.einsum("sqhd,skhd->shqk", queries, keys, preferred_element_type=jnp.float32)
            * factor
        )
        highest = jnp.maximum(running, jnp.max(scores, axis=-1))
        shrink = jnp.exp(running - highest)
        weights = jnp.exp(scores - highest[..., None])
        denom = denom * shrink + jnp.sum(weights, axis=-1)
        accum = accum * shrink[..., None] + jnp.einsum(
            "shqk,skhd->shqd",
            weights.astype(jnp.bfloat16),
            values,
            preferred_element_type=jnp.float32,
        )
        return (highest, denom, accum)

    return lax.fori_loop(0, piece_rows // size, attend_one_block, carry)


def block_grads(block, queries, grad_out, logsum, delta, width, factor):
    keys, values = split_kv(block, width)
    scores = (
        jnp.einsum("sqhd,skhd->shqk", queries, keys, preferred_element_type=jnp.float32) * factor
    )
    probs = jnp.exp(scores - logsum[..., None])
    dprobs = jnp.einsum("sqhd,skhd->shqk", grad_out, values, preferred_element_type=jnp.float32)
    dscores = (probs * (dprobs - delta[..., None])).astype(jnp.bfloat16)
    return (keys, probs, dscores)


def query_grads(kv_all, queries, grad_out, logsum, delta, width, factor):
    total_rows = kv_all.shape[1]
    size = math.gcd(total_rows, 512)

    def query_one_block(index, accum):
        block = lax.dynamic_slice_in_dim(kv_all, index * size, size, 1)
        keys, probs, dscores = block_grads(block, queries, grad_out, logsum, delta, width, factor)
        return accum + factor * jnp.einsum(
            "shqk,skhd->sqhd", dscores, keys, preferred_element_type=jnp.float32
        )

    return lax.fori_loop(
        0, total_rows // size, query_one_block, jnp.zeros(queries.shape, jnp.float32)
    )


def key_grads(kv_all, queries, grad_out, logsum, delta, width, factor, count):
    size = math.gcd(count, 512)
    seqs = queries.shape[0]

    def key_one_block(index, accum):
        block = lax.dynamic_slice_in_dim(kv_all, index * size, size, 1)
        keys, probs, dscores = block_grads(block, queries, grad_out, logsum, delta, width, factor)
        grad_vals = jnp.einsum(
            "shqk,sqhd->skhd",
            probs.astype(jnp.bfloat16),
            grad_out,
            preferred_element_type=jnp.float32,
        )
        grad_keys = factor * jnp.einsum(
            "shqk,sqhd->skhd", dscores, queries, preferred_element_type=jnp.float32
        )
        joined = jnp.concatenate(
            [grad_keys.reshape(seqs, size, width), grad_vals.reshape(seqs, size, width)], axis=-1
        )
        return lax.dynamic_update_slice_in_dim(
            accum, jnp.transpose(joined, (1, 0, 2)), index * size, 0
        )

    initial = jnp.zeros((count, seqs, 2 * width), jnp.float32)
    return lax.fori_loop(0, count // size, key_one_block, initial)


def adam_step(weight, grad, first, second, rate, decay_rate):
    new_first = BETA_ONE * first + (1.0 - BETA_ONE) * grad
    new_second = BETA_TWO * second + (1.0 - BETA_TWO) * grad * grad
    fixed_first = new_first / (1.0 - BETA_ONE**STEP)
    fixed_second = new_second / (1.0 - BETA_TWO**STEP)
    new_weight = weight - rate * (
        fixed_first / (jnp.sqrt(fixed_second) + ADAM_EPS) + decay_rate * weight
    )
    return (new_first, new_second, new_weight)


def mod_back(grad_hidden, ln_values, normed, scale_part, gain):
    grad_shift = jnp.sum(grad_hidden, axis=1)
    grad_scale = jnp.sum(grad_hidden * ln_values, axis=1)
    grad_ln = grad_hidden * (1.0 + scale_part)
    grad_gain = jnp.sum(grad_ln * normed, axis=(0, 1))
    return (grad_shift, grad_scale, grad_gain, grad_ln * gain)


def plain(
    tokens_in,
    cotangent,
    timesteps,
    span_start,
    span_len,
    vectors,
    w_ada,
    w_qkv,
    w_attn,
    w_in,
    w_out,
    m_vec,
    v_vec,
    m_ada,
    v_ada,
    m_qkv,
    v_qkv,
    m_attn,
    v_attn,
    m_in,
    v_in,
    m_out,
    v_out,
):
    seqs, group, width = tokens_in.shape
    heads = width // HD
    factor = HD ** (-0.5)
    flat_rows = seqs * group
    full_ada, full_qkv, full_attn, full_in, full_out = (
        lax.all_gather(w_ada.astype(jnp.bfloat16), ("dp", "seq"), axis=1, tiled=True),
        lax.all_gather(w_qkv.astype(jnp.bfloat16), ("dp", "seq"), axis=0, tiled=True),
        lax.all_gather(w_attn.astype(jnp.bfloat16), ("dp", "seq"), axis=0, tiled=True),
        lax.all_gather(w_in.astype(jnp.bfloat16), ("dp", "seq"), axis=0, tiled=True),
        lax.all_gather(w_out.astype(jnp.bfloat16), ("dp", "seq"), axis=0, tiled=True),
    )
    positions = lax.axis_index("seq") * group + jnp.arange(group, dtype=jnp.int32)
    masked = (positions[None, :] >= span_start[:, None]) & (
        positions[None, :] < (span_start + span_len)[:, None]
    )
    cond_bf = cond_input(timesteps).astype(jnp.bfloat16)
    modulation = jnp.dot(cond_bf, full_ada, preferred_element_type=jnp.float32) + vectors[
        2:8
    ].reshape(1, 6 * width)
    pieces = [modulation[:, which * width : (which + 1) * width][:, None, :] for which in range(6)]
    shift_one, scale_one, gate_one, shift_two, scale_two, gate_two = pieces
    start_tokens = jnp.where(
        masked[..., None], vectors[8][None, None, :], tokens_in.astype(jnp.float32)
    )
    normed_one, inv_one = normalize(start_tokens)
    ln_one = normed_one * vectors[0]
    hidden_one = (
        (ln_one * (1.0 + scale_one) + shift_one).astype(jnp.bfloat16).reshape(flat_rows, width)
    )
    projected = jnp.dot(hidden_one, full_qkv, preferred_element_type=jnp.float32).reshape(
        seqs, group, 3 * width
    )
    cosines, sines = rotary_tables(positions)
    queries = rotate(projected[..., :width].reshape(seqs, group, heads, HD), cosines, sines).astype(
        jnp.bfloat16
    )
    keys_here = rotate(
        projected[..., width : 2 * width].reshape(seqs, group, heads, HD), cosines, sines
    ).astype(jnp.bfloat16)
    values_here = projected[..., 2 * width :].astype(jnp.bfloat16)
    kv_local = jnp.concatenate([keys_here.reshape(seqs, group, width), values_here], axis=-1)
    initial = (
        jnp.full((seqs, heads, group), -1e30, jnp.float32),
        jnp.zeros((seqs, heads, group), jnp.float32),
        jnp.zeros((seqs, heads, group, HD), jnp.float32),
    )
    running, denom, accum = attend_piece(
        initial, lax.all_gather(kv_local, "seq", axis=1, tiled=True), queries, width, factor
    )
    attn_heads = accum / denom[..., None]
    logsum = running + jnp.log(denom)
    attn_rows = jnp.transpose(attn_heads, (0, 2, 1, 3)).reshape(flat_rows, width)
    attn_bf = attn_rows.astype(jnp.bfloat16)
    branch_one = jnp.dot(attn_bf, full_attn, preferred_element_type=jnp.float32).reshape(
        seqs, group, width
    )
    mid_tokens = start_tokens + gate_one * branch_one
    normed_two, inv_two = normalize(mid_tokens)
    ln_two = normed_two * vectors[1]
    hidden_two = (
        (ln_two * (1.0 + scale_two) + shift_two).astype(jnp.bfloat16).reshape(flat_rows, width)
    )
    pre_act = jnp.dot(hidden_two, full_in, preferred_element_type=jnp.float32)
    activ, gelu_back = jax.vjp(partial(jax.nn.gelu, approximate=True), pre_act)
    activ_bf = activ.astype(jnp.bfloat16)
    branch_two = jnp.dot(activ_bf, full_out, preferred_element_type=jnp.float32).reshape(
        seqs, group, width
    )
    block_out = (mid_tokens + gate_two * branch_two).astype(jnp.bfloat16)
    grad_y = cotangent.astype(jnp.float32)
    grad_gate_two = jnp.sum(grad_y * branch_two, axis=1)
    grad_branch_two = (grad_y * gate_two).astype(jnp.bfloat16).reshape(flat_rows, width)
    grad_w_out = jnp.dot(activ_bf.T, grad_branch_two, preferred_element_type=jnp.float32)
    grad_activ = jnp.dot(grad_branch_two, full_out.T, preferred_element_type=jnp.float32)
    grad_pre = gelu_back(grad_activ)[0].astype(jnp.bfloat16)
    grad_w_in = jnp.dot(hidden_two.T, grad_pre, preferred_element_type=jnp.float32)
    grad_hidden_two = jnp.dot(grad_pre, full_in.T, preferred_element_type=jnp.float32).reshape(
        seqs, group, width
    )
    grad_shift_two, grad_scale_two, grad_gain_two, grad_normed_two = mod_back(
        grad_hidden_two, ln_two, normed_two, scale_two, vectors[1]
    )
    grad_mid = grad_y + norm_back(normed_two, inv_two, grad_normed_two)
    grad_gate_one = jnp.sum(grad_mid * branch_one, axis=1)
    grad_branch_one = (grad_mid * gate_one).astype(jnp.bfloat16).reshape(flat_rows, width)
    grad_w_attn = jnp.dot(attn_bf.T, grad_branch_one, preferred_element_type=jnp.float32)
    grad_attn_bf = (
        jnp.dot(grad_branch_one, full_attn.T, preferred_element_type=jnp.float32)
        .astype(jnp.bfloat16)
        .reshape(seqs, group, heads, HD)
    )
    delta = jnp.einsum("sqhd,shqd->shq", grad_attn_bf.astype(jnp.float32), attn_heads)
    kv_all = lax.all_gather(kv_local, "seq", axis=1, tiled=True)
    grad_queries = query_grads(kv_all, queries, grad_attn_bf, logsum, delta, width, factor)
    grad_kv = jnp.transpose(
        lax.psum_scatter(
            key_grads(
                kv_all,
                queries,
                grad_attn_bf,
                logsum,
                delta,
                width,
                factor,
                group * lax.axis_size("seq"),
            ).astype(jnp.bfloat16),
            "seq",
            scatter_dimension=0,
            tiled=True,
        ).astype(jnp.float32),
        (1, 0, 2),
    )
    grad_keys = grad_kv[..., :width].reshape(seqs, group, heads, HD)
    grad_qkv = jnp.concatenate(
        [
            rotate_back(grad_queries, cosines, sines).reshape(seqs, group, width),
            rotate_back(grad_keys, cosines, sines).reshape(seqs, group, width),
            grad_kv[..., width:],
        ],
        axis=-1,
    )
    grad_qkv = grad_qkv.astype(jnp.bfloat16).reshape(flat_rows, 3 * width)
    grad_w_qkv = jnp.dot(hidden_one.T, grad_qkv, preferred_element_type=jnp.float32)
    grad_hidden_one = jnp.dot(grad_qkv, full_qkv.T, preferred_element_type=jnp.float32).reshape(
        seqs, group, width
    )
    grad_shift_one, grad_scale_one, grad_gain_one, grad_normed_one = mod_back(
        grad_hidden_one, ln_one, normed_one, scale_one, vectors[0]
    )
    grad_start = grad_mid + norm_back(normed_one, inv_one, grad_normed_one)
    grad_mask_row = jnp.sum(jnp.where(masked[..., None], grad_start, 0.0), axis=(0, 1))
    grad_input = jnp.where(masked[..., None], 0.0, grad_start)
    grad_mod = jnp.concatenate(
        [
            grad_shift_one,
            grad_scale_one,
            grad_gate_one,
            grad_shift_two,
            grad_scale_two,
            grad_gate_two,
        ],
        axis=1,
    )
    grad_w_ada = jnp.dot(cond_bf.astype(jnp.float32).T, grad_mod, precision=lax.Precision.HIGHEST)
    grad_vectors = jnp.concatenate(
        [
            grad_gain_one[None, :],
            grad_gain_two[None, :],
            jnp.sum(grad_mod, axis=0).reshape(6, width),
            grad_mask_row[None, :],
        ],
        axis=0,
    )
    red_ada, red_qkv, red_attn, red_in, red_out, red_vec = (
        lax.psum_scatter(grad_w_ada, ("dp", "seq"), scatter_dimension=1, tiled=True),
        lax.psum_scatter(grad_w_qkv, ("dp", "seq"), scatter_dimension=0, tiled=True),
        lax.psum_scatter(grad_w_attn, ("dp", "seq"), scatter_dimension=0, tiled=True),
        lax.psum_scatter(grad_w_in, ("dp", "seq"), scatter_dimension=0, tiled=True),
        lax.psum_scatter(grad_w_out, ("dp", "seq"), scatter_dimension=0, tiled=True),
        lax.psum_scatter(grad_vectors, ("dp", "seq"), scatter_dimension=1, tiled=True),
    )
    local_squares = jnp.float32(0.0)
    for reduced in (red_vec, red_ada, red_qkv, red_attn, red_in, red_out):
        local_squares = local_squares + jnp.sum(reduced * reduced)
    grad_norm = jnp.sqrt(lax.psum(local_squares, ("dp", "seq")))
    clip_factor = jnp.minimum(1.0, CLIP / (grad_norm + 1e-06))
    columns = red_vec.shape[1]
    own_vectors = lax.dynamic_slice_in_dim(
        vectors, lax.axis_index(("dp", "seq")) * columns, columns, 1
    )
    vec_out = adam_step(own_vectors, red_vec * clip_factor, m_vec, v_vec, RATE_VECTORS, 0.0)
    ada_out = adam_step(w_ada, red_ada * clip_factor, m_ada, v_ada, RATE, DECAY)
    qkv_out = adam_step(w_qkv, red_qkv * clip_factor, m_qkv, v_qkv, RATE, DECAY)
    attn_out = adam_step(w_attn, red_attn * clip_factor, m_attn, v_attn, RATE, DECAY)
    in_out = adam_step(w_in, red_in * clip_factor, m_in, v_in, RATE, DECAY)
    out_out = adam_step(w_out, red_out * clip_factor, m_out, v_out, RATE, DECAY)
    return (
        block_out,
        grad_input,
        grad_norm,
        vec_out[0],
        vec_out[1],
        vec_out[2],
        ada_out[0],
        ada_out[1],
        ada_out[2],
        qkv_out[0],
        qkv_out[1],
        qkv_out[2],
        attn_out[0],
        attn_out[1],
        attn_out[2],
        in_out[0],
        in_out[1],
        in_out[2],
        out_out[0],
        out_out[1],
        out_out[2],
    )


F32, BF = jnp.float32, jnp.bfloat16
MESH = pl.DeviceIdType.MESH
DP, LINE, SEQ, CHIPS, ALL = 4, 4, 8, 16, 32
ROWS, WIDTH, PACK = 128, 768, 640
HALF = WIDTH // 2
HALVES = ((0, 0), (0, 1), (0, 2), (2, 2), (1, 0), (1, 1), (1, 2), None, (2, 0), (2, 1))

def numbered(**counts):
    at = {}
    for name, count in counts.items():
        at[name] = sum(counts[other] for other in at)
    return SimpleNamespace(**at), sum(counts.values())


S, SEM_COUNT = numbered(
    cond=1,
    mix_qkv=1,
    mix_in=1,
    mix_attn=1,
    mod=1,
    w_qkv=1,
    w_attn=1,
    w_in=1,
    w_out=1,
    group_qkv=1,
    group_attn=1,
    fw_qkv=1,
    fw_attn=1,
    fw_in=1,
    fw_out=1,
    h1=4,
    h2=4,
    dm=4,
    xf=4,
    o=1,
    mm=1,
    dh2=1,
    do=1,
    gp=1,
    dh1=1,
    pair_out=1,
    pair_in=1,
    pair_attn=1,
    pair_qkv=1,
    plane_attn=1,
    plane_qkv=1,
    line_out=1,
    line_in=1,
    line_attn=1,
    line_qkv=1,
    last_in=1,
    last_attn=1,
    last_qkv=1,
    early=1,
    early2=1,
    late=1,
    late2=1,
    sq=1,
)

SCRATCH = dict(
    wide_qkv=((48, 3072), F32),
    wide_in=((48, 3072), F32),
    wide_attn=((48, 768), F32),
    s_qkv=((48, 3072), BF),
    s_in=((48, 3072), BF),
    s_attn=((48, 768), BF),
    s_out=((96, 768), BF),
    w_qkv=((768, 768), BF),
    w_in=((768, 768), BF),
    w_attn=((768, 768), BF),
    w_out=((4, 2, 96, 768), BF),
    conds_all=((4, 8, 128), F32),
    mod_send=((4, 4, 128), F32),
    mod_got=((32, 4, 128), F32),
    mod_flat=((40, 128), F32),
    mod=((8, 768), F32),
    x0=((128, 768), F32),
    n1=((128, 768), F32),
    inv1=((128, 128), F32),
    x1=((128, 768), F32),
    n2=((128, 768), F32),
    inv2=((128, 128), F32),
    a=((128, 768), F32),
    dx1=((128, 768), F32),
    h1=((4, 128, 768), BF),
    h2=((4, 128, 768), BF),
    dm=((4, 128, 768), BF),
    gb=((4, 128, 768), BF),
    du=((4, 128, 768), BF),
    xb=((2, 4, 128, 640), BF),
    pt=((3, 1024, 512), BF),
    ot=((2, 128, 512), F32),
    os=((4, 128, 256), BF),
    ob=((4, 128, 256), BF),
    mms=((4, 128, 768), BF),
    mmr=((4, 128, 768), BF),
    dhs=((4, 128, 768), BF),
    dhr=((4, 128, 768), BF),
    das=((128, 768), BF),
    dos=((4, 128, 256), BF),
    dob=((4, 128, 256), BF),
    dst=((1024, 512), BF),
    ga=((1024, 640), F32),
    gps=((512, 512), BF),
    gpr=((512, 512), BF),
    dqkv=((4, 128, 768), BF),
    d1s=((4, 128, 768), BF),
    d1r=((4, 128, 768), BF),
    g_out=((4, 2, 96, 768), BF),
    g_in=((2, 768, 384), BF),
    g_attn=((2, 768, 384), BF),
    g_qkv=((2, 768, 384), BF),
    p_out=((4, 96, 768), BF),
    p_in=((768, 384), BF),
    p_attn=((768, 384), BF),
    p_qkv=((768, 384), BF),
    q_attn=((4, 192, 384), BF),
    q_qkv=((4, 192, 384), BF),
    m_attn=((192, 384), BF),
    m_qkv=((192, 384), BF),
    r_out=((4, 96, 768), BF),
    r_in=((16, 48, 384), BF),
    r_attn=((4, 48, 384), BF),
    r_qkv=((4, 48, 384), BF),
    t_in=((4, 48, 384), F32),
    t_attn=((1, 48, 384), F32),
    t_qkv=((4, 48, 384), F32),
    f_in=((4, 2, 24, 384), F32),
    f_attn=((1, 2, 24, 384), F32),
    f_qkv=((4, 2, 24, 384), F32),
    early=((8, 768), F32),
    early_got=((8, 8, 768), F32),
    early_all=((4, 8, 768), F32),
    late=((4, 768), F32),
    late_got=((8, 4, 768), F32),
    late_all=((4, 4, 768), F32),
    sq=((32, 1, 128), F32),
)


def dot(left, right):
    return jnp.dot(left, right, preferred_element_type=F32)


def dot_nt(left, right):
    return lax.dot_general(left, right, (((1,), (1,)), ((), ())), preferred_element_type=F32)


def dot_tn(left, right):
    return lax.dot_general(left, right, (((0,), (0,)), ((), ())), preferred_element_type=F32)


def loop(count, body, start=0):
    def step(index, carry):
        body(index)
        return carry

    lax.fori_loop(start, count, step, 0)


def layer_kernel(
    i_tok,
    i_cot,
    i_cond,
    i_hide,
    i_vec,
    i_wada,
    i_wqkv,
    i_wattn,
    i_win,
    i_wout,
    i_turn,
    o_y,
    o_dx,
    o_norm,
    o_gqkv,
    o_gattn,
    o_gin,
    o_gout,
    o_dmod,
    o_gvec,
    o_conds,
    *scratch,
):
    r = SimpleNamespace(**dict(zip(SCRATCH, scratch)))
    send_sems, recv_sems = scratch[-2:]
    b, s = lax.axis_index("dp"), lax.axis_index("seq")
    z, c = lax.div(s, 2), lax.rem(s, 2)
    mate = s + 1 - 2 * c
    chip = b * LINE + z
    me = b * SEQ + s
    drains = []

    def push(src, dst, at, to_b, to_s):
        pltpu.make_async_remote_copy(
            src_ref=src,
            dst_ref=dst,
            send_sem=send_sems.at[at],
            recv_sem=recv_sems.at[at],
            device_id=(to_b, to_s),
            device_id_type=MESH,
        ).start()

    def keep(src, dst, at):
        pltpu.make_async_copy(src, dst, recv_sems.at[at]).start()

    def got(at, like):
        pltpu.make_async_copy(like, like, recv_sems.at[at]).wait()

    def left(at, like):
        pltpu.make_async_copy(like, like, send_sems.at[at]).wait()

    def sent(at, like):
        drains.append((at, like))

    def peers(body):
        for k in (1, 2, 3):
            body(lax.rem(b + k, DP))

    def stack(body):
        for k in (1, 2, 3):
            body(lax.rem(z + k, LINE))

    lane = lax.broadcasted_iota(jnp.int32, (1, 128), 1)
    low = lane < 64
    own24 = pl.ds(pl.multiple_of(24 * c, 8), 24)
    mate24 = pl.ds(pl.multiple_of(24 * (1 - c), 8), 24)
    part = pl.ds(pl.multiple_of(HALF * c, 128), HALF)
    chip_rows = pl.ds(pl.multiple_of(48 * chip, 16), 48)
    group_rows = pl.ds(pl.multiple_of(192 * b, 16), 192)

    barrier = pltpu.get_barrier_semaphore()

    def greet(k):
        other = lax.rem(me + k, ALL)
        pl.semaphore_signal(
            barrier, inc=1, device_id=(lax.div(other, SEQ), lax.rem(other, SEQ)), device_id_type=MESH
        )

    loop(ALL, greet, 1)

    def natural(kind, p, head):
        return kind * WIDTH + 192 * p + 64 * head

    def half_at(ref, column, high):
        tile = ref[:, column // 128 * 128 : column // 128 * 128 + 128]
        return tile if (column % 128 == 64) == high else pltpu.roll(tile, 64, 1)

    for p in range(4):
        for tile in range(5):
            pair = []
            for high in (0, 1):
                which = HALVES[2 * tile + high]
                pair.append(
                    jnp.zeros((24, 128), F32)
                    if which is None
                    else half_at(i_wqkv, natural(which[0], p, which[1]), bool(high))
                )
            r.wide_qkv[own24, 768 * p + 128 * tile : 768 * p + 128 * tile + 128] = jnp.where(
                low, pair[0], pair[1]
            )
        r.wide_qkv[own24, 768 * p + 640 : 768 * p + 768] = jnp.zeros((24, 128), F32)
    r.wide_in[own24, :] = i_win[...]
    r.wide_attn[own24, :] = i_wattn[...]
    r.s_out[...] = i_wout[...].astype(BF)
    r.conds_all[b] = i_cond[...]
    pl.semaphore_wait(barrier, ALL - 1)

    def stack_rows(to):
        push(r.s_out, r.w_out.at[z, c], S.w_out, b, 2 * to + c)

    peers(lambda to: push(r.conds_all.at[b], r.conds_all.at[b], S.cond, to, s))
    sent(S.cond, r.conds_all.at[0:3])
    push(r.wide_qkv.at[own24], r.wide_qkv.at[own24], S.mix_qkv, b, mate)
    sent(S.mix_qkv, r.wide_qkv.at[0:24])
    push(r.wide_attn.at[own24], r.wide_attn.at[own24], S.mix_attn, b, mate)
    sent(S.mix_attn, r.wide_attn.at[0:24])
    push(r.wide_in.at[own24], r.wide_in.at[own24], S.mix_in, b, mate)
    sent(S.mix_in, r.wide_in.at[0:24])
    stack(stack_rows)
    keep(r.s_out, r.w_out.at[z, c], S.w_out)
    sent(S.w_out, r.w_out.at[0:3, 0])

    got(S.cond, r.conds_all.at[0:3])
    row8 = lax.broadcasted_iota(jnp.int32, (8, 128), 0)
    cond4 = jnp.zeros((8, 128), F32)
    for k in range(4):
        cond4 = jnp.where(row8 == k, r.conds_all[k], cond4)
    o_conds[...] = cond4
    columns = dot(cond4.astype(BF), i_wada[...])
    columns = pltpu.roll(columns, lax.rem(144 * me, 128), 1)
    for k in range(4):
        for t in range(3):
            r.mod_send[k, t : t + 1, :] = columns[k : k + 1, 128 * t : 128 * t + 128]
        r.mod_send[k, 3:4, :] = jnp.zeros((1, 128), F32)

    def send_mod(k):
        other = lax.rem(me + k, ALL)
        ob = lax.div(other, SEQ)
        push(r.mod_send.at[ob], r.mod_got.at[me], S.mod, ob, lax.rem(other, SEQ))

    loop(ALL, send_mod, 1)
    sent(S.mod, r.mod_got.at[0:31])
    keep(r.mod_send.at[b], r.mod_got.at[me], S.mod)

    def block(src, first):
        return src.at[:, pl.ds(pl.multiple_of(first, 128), HALF)]

    def spread(src, dst, at):
        def one(k):
            to = lax.rem(chip + k, CHIPS)
            to_b, to_z = lax.div(to, LINE), lax.rem(to, LINE)
            push(
                block(src, WIDTH * to_b + HALF * c),
                dst.at[chip_rows, part],
                at,
                to_b,
                2 * to_z + c,
            )

        loop(CHIPS, one, 1)
        keep(block(src, WIDTH * b + HALF * c), dst.at[chip_rows, part], at)
        sent(at, dst.at[0:720, 0:HALF])

    def along_line(src, dst, at, step):
        stack(
            lambda to: push(
                block(src, step * to + HALF * c), dst.at[chip_rows, part], at, b, 2 * to + c
            )
        )
        keep(block(src, step * z + HALF * c), dst.at[chip_rows, part], at)
        sent(at, dst.at[0:144, 0:HALF])

    def over_plane(dst, first, at):
        got(first, dst.at[0:192, 0:HALF])
        peers(
            lambda to: push(dst.at[group_rows, part], dst.at[group_rows, part], at, to, s)
        )
        sent(at, dst.at[0:576, 0:HALF])

    def share(dst, at, onward, rows):
        got(at, dst.at[0:rows, 0:HALF])
        push(dst.at[:, part], dst.at[:, part], onward, b, mate)
        sent(onward, dst.at[:, 0:HALF])

    got(S.mix_qkv, r.wide_qkv.at[0:24])
    r.s_qkv[...] = r.wide_qkv[...].astype(BF)
    along_line(r.s_qkv, r.w_qkv, S.w_qkv, WIDTH)
    got(S.mix_attn, r.wide_attn.at[0:24])
    r.s_attn[...] = r.wide_attn[...].astype(BF)
    along_line(r.s_attn, r.w_attn, S.w_attn, 0)

    hidden = i_hide[:, 0:1] > 0.5
    x0 = jnp.where(hidden, i_vec[8:9, :], i_tok[...].astype(F32))
    r.x0[...] = x0
    n1, inv1 = normalize(x0)
    r.n1[...] = n1
    r.inv1[...] = jnp.broadcast_to(inv1, (ROWS, 128))

    got(S.mod, r.mod_got)
    r.mod_flat[...] = jnp.zeros((40, 128), F32)
    for k in range(ALL):
        first = 9 * k // 8
        r.mod_flat[first : first + 3, :] += r.mod_got[k, 0:3, :]
    for k in range(6):
        row = jnp.concatenate(
            [r.mod_flat[6 * k + t : 6 * k + t + 1, :] for t in range(6)], axis=1
        )
        r.mod[k : k + 1, :] = row + i_vec[2 + k : 3 + k, :]

    def mod(k):
        return r.mod[k : k + 1, :]

    def vec(k):
        return i_vec[k : k + 1, :]

    r.h1[z] = (r.n1[...] * vec(0) * (1.0 + mod(1)) + mod(0)).astype(BF)
    stack(lambda to: push(r.h1.at[z], r.h1.at[z], S.h1 + z, b, 2 * to + c))
    sent(S.h1 + z, r.h1.at[0:3])
    r.dm[b] = (i_cot[...].astype(F32) * mod(5)).astype(BF)
    over_plane(r.w_qkv, S.w_qkv, S.group_qkv)
    got(S.mix_in, r.wide_in.at[0:24])
    r.s_in[...] = r.wide_in[...].astype(BF)

    share(r.w_qkv, S.group_qkv, S.fw_qkv, 576)
    over_plane(r.w_attn, S.w_attn, S.group_attn)
    peers(lambda to: push(r.dm.at[b], r.dm.at[b], S.dm + b, to, s))
    sent(S.dm + b, r.dm.at[0:3])
    got(S.fw_qkv, r.w_qkv.at[:, 0:HALF])

    def turned(tile, sign, k):
        return tile * i_turn[0, k] + sign * (
            pltpu.roll(tile, 96, 1) * i_turn[1, k] + pltpu.roll(tile, 32, 1) * i_turn[2, k]
        )

    def project(j):
        k = lax.rem(z + j, LINE)

        @pl.when(j > 0)
        def _():
            got(S.h1 + k, r.h1.at[0])

        x = dot(r.h1[k], r.w_qkv[:, 0:PACK])
        tiles = [x[:, 128 * t : 128 * t + 128] for t in range(5)]
        tiles[0] = turned(tiles[0], 1.0, k) * 0.125
        tiles[1] = jnp.where(low, turned(tiles[1], 1.0, k) * 0.125, tiles[1])
        tiles[2] = turned(tiles[2], 1.0, k)
        tiles[3] = turned(tiles[3], 1.0, k)
        for t in range(5):
            r.xb[0, k, :, 128 * t : 128 * t + 128] = tiles[t].astype(BF)
        push(r.xb.at[0, k], r.xb.at[1, k], S.xf + k, b, mate)

    loop(4, project)
    for k in range(4):
        sent(S.xf + k, r.xb.at[0, 0])

    spread(r.s_in, r.w_in, S.w_in)
    for k in range(4):
        got(S.xf + k, r.xb.at[0, 0])

    def tile_of(t):
        return r.xb[:, :, :, 128 * t : 128 * t + 128].reshape(1024, 128)

    heads = ((0, 2, 4, True, True), (0, 2, 4, False, False), (1, 3, 1, True, False))

    def queries(head, first, size):
        q_tile, _, _, q_low, _ = heads[head]
        q = r.xb[0, first : first + size, :, 128 * q_tile : 128 * q_tile + 128]
        return jnp.where(low if q_low else ~low, q.reshape(size * 128, 128), jnp.zeros((), BF))

    for head in range(3):
        keys, values = tile_of(heads[head][1]), tile_of(heads[head][2])
        for half in range(2):
            at = slice(256 * half, 256 * half + 256)
            scores = dot_nt(keys, queries(head, 2 * half, 2))
            weights = jnp.exp(scores - jnp.max(scores, axis=0, keepdims=True))
            weights = weights * (1.0 / jnp.sum(weights, axis=0, keepdims=True))
            weights = weights.astype(BF)
            r.pt[head, :, at] = weights
            out = dot_tn(values, weights)
            if head == 0:
                r.ot[0, 0:64, at] = out[0:64]
            elif head == 1:
                r.ot[0, 64:128, at] = out[64:128]
            else:
                r.ot[1, 0:64, at] = out[64:128]
                r.ot[1, 64:128, at] = jnp.zeros((64, 256), F32)
    for t in range(2):
        r.os[:, :, 128 * t : 128 * t + 128] = (
            r.ot[t].T.astype(BF).reshape(4, 128, 128)
        )

    stack(lambda to: push(r.os.at[to], r.ob.at[z], S.o, b, 2 * to + c))
    keep(r.os.at[z], r.ob.at[z], S.o)
    sent(S.o, r.os.at[0:3])
    share(r.w_attn, S.group_attn, S.fw_attn, 576)
    got(S.fw_attn, r.w_attn.at[:, 0:HALF])
    got(S.o, r.ob)
    a = jnp.zeros((ROWS, WIDTH), F32)
    for p in range(4):
        a += dot(r.ob[p, :, 0:128], r.w_attn[192 * p : 192 * p + 128, :])
        a += dot(r.ob[p, :, 128:192], r.w_attn[192 * p + 128 : 192 * p + 192, :])
    r.a[...] = a
    x1 = r.x0[...] + mod(2) * a
    r.x1[...] = x1
    n2, inv2 = normalize(x1)
    r.n2[...] = n2
    r.inv2[...] = jnp.broadcast_to(inv2, (ROWS, 128))
    r.h2[b] = (n2 * vec(1) * (1.0 + mod(4)) + mod(3)).astype(BF)
    peers(lambda to: push(r.h2.at[b], r.h2.at[b], S.h2 + b, to, s))
    sent(S.h2 + b, r.h2.at[0:3])
    got(S.w_out, r.w_out.at[:, 0])
    push(r.w_out.at[:, c], r.w_out.at[:, c], S.fw_out, b, mate)
    sent(S.fw_out, r.w_out.at[:, 0])
    share(r.w_in, S.w_in, S.fw_in, 768)
    got(S.fw_out, r.w_out.at[:, 0])
    got(S.fw_in, r.w_in.at[:, 0:HALF])

    def feed(j):
        k = lax.rem(b + j, DP)

        @pl.when(j > 0)
        def _():
            got(S.h2 + k, r.h2.at[0])
            got(S.dm + k, r.dm.at[0])

        u = dot(r.h2[k], r.w_in[...])
        slope = 0.7978845608028654
        cube = 0.044715
        t = jnp.tanh(slope * (u + cube * u * u * u))
        r.gb[k] = (0.5 * u * (1.0 + t)).astype(BF)
        bend = 0.5 * (1.0 + t) + 0.5 * u * (1.0 - t * t) * (slope * (1.0 + 3.0 * cube * u * u))
        r.du[k] = (dot_nt(r.dm[k], r.w_out[...].reshape(768, 768)) * bend).astype(BF)
        r.dhs[k] = dot_nt(r.du[k], r.w_in[...]).astype(BF)

        @pl.when(j > 0)
        def _():
            push(r.dhs.at[k], r.dhr.at[b], S.dh2, k, s)

    loop(4, feed)
    sent(S.dh2, r.dhs.at[0:3])

    def feed_out(j):
        k = lax.rem(b + j, DP)
        r.mms[k] = dot(r.gb[k], r.w_out[...].reshape(768, 768)).astype(BF)

        @pl.when(j > 0)
        def _():
            push(r.mms.at[k], r.mmr.at[b], S.mm, k, s)

    loop(4, feed_out)
    sent(S.mm, r.mms.at[0:3])

    def gather(own, others):
        total = own[b].astype(F32)
        for k in (1, 2, 3):
            total += others[lax.rem(b + k, DP)].astype(F32)
        return total

    for k in range(4):
        rows = slice(192 * k, 192 * k + 192)
        block = dot_tn(r.gb[:, :, rows].reshape(512, 192), r.dm[...].reshape(512, 768))
        r.g_out[k] = block.astype(BF).reshape(2, 96, 768)
    push(r.g_out.at[:, 1 - c], r.p_out, S.pair_out, b, mate)
    sent(S.pair_out, r.p_out)

    def outer(left, right, dst):
        def one(k):
            rows = pl.ds(pl.multiple_of(128 * k, 128), 128)
            result = dot_tn(
                left[:, :, rows].reshape(512, 128), right[...].reshape(512, 768)
            ).astype(BF)
            dst[0, rows, :] = result[:, 0:HALF]
            dst[1, rows, :] = result[:, HALF:WIDTH]

        loop(6, one)

    def to_mate(grad, dst, at):
        push(grad.at[1 - c], dst, at, b, mate)
        sent(at, dst)

    def pair_sum(grad, pair, at):
        got(at, pair)
        grad[c] = (grad[c].astype(F32) + pair[...].astype(F32)).astype(BF)

    def plane_sum(grad, dst, at):
        def rows(to):
            return grad.at[c, pl.ds(pl.multiple_of(192 * to, 16), 192)]

        peers(lambda to: push(rows(to), dst.at[b], at, to, s))
        keep(rows(b), dst.at[b], at)
        sent(at, dst.at[0:3])

    def line_sum(src, total, dst, first, at):
        got(first, src)
        total[...] = (
            (src[0].astype(F32) + src[1].astype(F32)) + (src[2].astype(F32) + src[3].astype(F32))
        ).astype(BF)

        def rows(to):
            return total.at[pl.ds(pl.multiple_of(48 * to, 16), 48)]

        stack(lambda to: push(rows(to), dst.at[z], at, b, 2 * to + c))
        keep(rows(z), dst.at[z], at)
        sent(at, dst.at[0:3])

    def trade(total, final, at):
        push(total.at[:, mate24], final.at[:, c], at, b, mate)
        sent(at, final.at[:, 0])
        final[:, c] = total[:, own24, :]

    outer(r.h2, r.du, r.g_in)
    to_mate(r.g_in, r.p_in, S.pair_in)

    got(S.pair_out, r.p_out)
    for k in range(4):
        r.g_out[k, c] = (r.g_out[k, c].astype(F32) + r.p_out[k].astype(F32)).astype(BF)

    def send_gout(to):
        push(r.g_out.at[to, c], r.r_out.at[z], S.line_out, b, 2 * to + c)

    stack(send_gout)
    keep(r.g_out.at[z, c], r.r_out.at[z], S.line_out)
    sent(S.line_out, r.r_out.at[0:3])

    got(S.dh2, r.dhr.at[0:3])
    dh = gather(r.dhs, r.dhr)
    n2 = r.n2[...]
    inv2 = r.inv2[:, 0:1]
    r.early[...] = jnp.zeros((8, 768), F32)
    r.early[2:3, :] = jnp.sum(dh, axis=0, keepdims=True)
    both = jnp.sum(dh * n2, axis=0, keepdims=True)
    r.early[3:4, :] = both * vec(1)
    r.early[0:1, :] = both * (1.0 + mod(4))
    grad = dh * ((1.0 + mod(4)) * vec(1))
    dx1 = i_cot[...].astype(F32) + norm_back(n2, inv2, grad)
    r.dx1[...] = dx1
    r.early[1:2, :] = jnp.sum(dx1 * r.a[...], axis=0, keepdims=True)
    r.das[...] = (dx1 * mod(2)).astype(BF)
    for p in range(4):
        first = 192 * p
        r.dos[p, :, 0:128] = dot_nt(r.das[...], r.w_attn[first : first + 128, :]).astype(BF)
        tail = dot_nt(r.das[...], r.w_attn[first + 128 : first + 192, :])
        r.dos[p, :, 128:256] = jnp.concatenate(
            [tail, jnp.zeros((ROWS, 64), F32)], axis=1
        ).astype(BF)

    stack(lambda to: push(r.dos.at[to], r.dob.at[z], S.do, b, 2 * to + c))
    keep(r.dos.at[z], r.dob.at[z], S.do)
    sent(S.do, r.dos.at[0:3])

    for p in range(4):
        rows = slice(192 * p, 192 * p + 192)
        result = dot_tn(r.ob[p], r.das[...])[0:192].astype(BF)
        r.g_attn[0, rows, :] = result[:, 0:HALF]
        r.g_attn[1, rows, :] = result[:, HALF:WIDTH]
    to_mate(r.g_attn, r.p_attn, S.pair_attn)

    got(S.mm, r.mmr.at[0:3])
    mm = gather(r.mms, r.mmr)
    o_y[...] = r.x1[...] + mod(5) * mm
    r.early[4:5, :] = jnp.sum(i_cot[...].astype(F32) * mm, axis=0, keepdims=True)

    def over_line(src, dst, name):
        def one(k):
            push(src, dst.at[s], name, b, lax.rem(s + k, SEQ))

        loop(SEQ, one, 1)
        keep(src, dst.at[s], name)
        sent(name, dst.at[0:7])

    def over_group(got_ref, dst, name):
        total = got_ref[0]
        for k in range(1, SEQ):
            total += got_ref[k]
        dst[b] = total
        peers(lambda to: push(dst.at[b], dst.at[b], name, to, s))
        sent(name, dst.at[0:3])

    over_line(r.early, r.early_got, S.early)

    pair_sum(r.g_in, r.p_in, S.pair_in)

    def send_gin(k):
        to = lax.rem(chip + k, CHIPS)
        push(
            r.g_in.at[c, pl.ds(pl.multiple_of(48 * to, 16), 48)],
            r.r_in.at[chip],
            S.line_in,
            lax.div(to, LINE),
            2 * lax.rem(to, LINE) + c,
        )

    loop(CHIPS, send_gin, 1)
    keep(r.g_in.at[c, chip_rows], r.r_in.at[chip], S.line_in)
    sent(S.line_in, r.r_in.at[0:15])
    pair_sum(r.g_attn, r.p_attn, S.pair_attn)
    plane_sum(r.g_attn, r.q_attn, S.plane_attn)

    got(S.do, r.dob)
    dot0, dot1 = r.dob[:, :, 0:128].reshape(512, 128), r.dob[:, :, 128:256].reshape(512, 128)
    zero = jnp.zeros((), BF)
    moved = pltpu.roll(dot1.astype(F32), 64, 1).astype(BF)
    grads = (jnp.where(low, dot0, zero), jnp.where(low, zero, dot0), moved)
    product = dot0.astype(F32).T * r.ot[0]
    deltas = (
        jnp.sum(product[0:64], axis=0, keepdims=True),
        jnp.sum(product[64:128], axis=0, keepdims=True),
        jnp.sum(dot1.astype(F32).T * r.ot[1], axis=0, keepdims=True),
    )
    turned_q = []
    for head in range(3):
        keys, values = tile_of(heads[head][1]), tile_of(heads[head][2])
        for half in range(2):
            at = slice(256 * half, 256 * half + 256)
            dp = dot_nt(values, grads[head][at])
            ds = (r.pt[head, :, at].astype(F32) * (dp - deltas[head][:, at])).astype(BF)
            r.dst[:, at] = ds
            turned_q.append(dot_tn(keys, ds))
        dk = dot(r.dst[...], queries(head, 0, 4))
        dv = dot(r.pt[head], grads[head])
        if head == 0:
            r.ga[:, 256:384] = dk
            r.ga[:, 512:640] = dv
        elif head == 1:
            r.ga[:, 256:384] += dk
            r.ga[:, 512:640] += dv
        else:
            r.ga[:, 384:512] = dk
            r.ga[:, 128:256] = dv
    r.gps[...] = r.ga[512:1024, 128:640].astype(BF)
    push(r.gps, r.gpr, S.gp, b, mate)
    sent(S.gp, r.gps)
    for half in range(2):
        at = slice(256 * half, 256 * half + 256)
        top = jnp.concatenate([turned_q[half][0:64], turned_q[2 + half][64:128]], axis=0)
        r.ga[at, 0:128] = top.T * 0.125
        r.ga[at, 128:256] += turned_q[4 + half].T * 0.125
    got(S.gp, r.gpr)

    def unproject(j):
        k = lax.rem(z + 1 + j, LINE)
        rows = pl.ds(pl.multiple_of(128 * k, 128), 128)
        tiles = [r.ga[rows, 0:128]] + [
            r.ga[rows, 128 * t : 128 * t + 128]
            + r.gpr[rows, 128 * t - 128 : 128 * t].astype(F32)
            for t in range(1, 5)
        ]
        tiles[0] = turned(tiles[0], -1.0, k)
        tiles[1] = jnp.where(low, turned(tiles[1], -1.0, k), tiles[1])
        tiles[2] = turned(tiles[2], -1.0, k)
        tiles[3] = turned(tiles[3], -1.0, k)
        for t in range(5):
            r.dqkv[k, :, 128 * t : 128 * t + 128] = tiles[t].astype(BF)
        r.dqkv[k, :, PACK:WIDTH] = jnp.zeros((128, 128), BF)
        r.d1s[k] = dot_nt(r.dqkv[k, :, 0:PACK], r.w_qkv[:, 0:PACK]).astype(BF)

        @pl.when(j < 3)
        def _():
            push(r.d1s.at[k], r.d1r.at[z], S.dh1, b, 2 * k + c)

    loop(4, unproject)
    sent(S.dh1, r.d1s.at[0:3])
    outer(r.h1, r.dqkv, r.g_qkv)
    to_mate(r.g_qkv, r.p_qkv, S.pair_qkv)
    line_sum(r.q_attn, r.m_attn, r.r_attn, S.plane_attn, S.line_attn)
    got(S.early, r.early_got)
    over_group(r.early_got, r.early_all, S.early2)
    pair_sum(r.g_qkv, r.p_qkv, S.pair_qkv)
    plane_sum(r.g_qkv, r.q_qkv, S.plane_qkv)

    got(S.line_in, r.r_in)
    for p in range(4):
        r.t_in[p] = (r.r_in[4 * p].astype(F32) + r.r_in[4 * p + 1].astype(F32)) + (
            r.r_in[4 * p + 2].astype(F32) + r.r_in[4 * p + 3].astype(F32)
        )
    trade(r.t_in, r.f_in, S.last_in)
    line_sum(r.q_qkv, r.m_qkv, r.r_qkv, S.plane_qkv, S.line_qkv)

    got(S.dh1, r.d1r.at[0:3])
    dh = r.d1s[z].astype(F32)
    for k in (1, 2, 3):
        dh += r.d1r[lax.rem(z + k, LINE)].astype(F32)
    n1 = r.n1[...]
    both = jnp.sum(dh * n1, axis=0, keepdims=True)
    r.late[0:1, :] = both * (1.0 + mod(1))
    r.late[1:2, :] = jnp.sum(dh, axis=0, keepdims=True)
    r.late[2:3, :] = both * vec(0)
    grad = dh * ((1.0 + mod(1)) * vec(0))
    dx0 = r.dx1[...] + norm_back(n1, r.inv1[:, 0:1], grad)
    o_dx[...] = dx0
    r.late[3:4, :] = jnp.sum(jnp.where(hidden, dx0, 0.0), axis=0, keepdims=True)
    over_line(r.late, r.late_got, S.late)

    got(S.line_out, r.r_out)
    total = (r.r_out[0].astype(F32) + r.r_out[1].astype(F32)) + (
        r.r_out[2].astype(F32) + r.r_out[3].astype(F32)
    )
    o_gout[...] = total
    squares = total * total
    squares = jnp.sum(squares[:, 0:128] + squares[:, 128:256] + squares[:, 256:384]
                      + squares[:, 384:512] + squares[:, 512:640] + squares[:, 640:768],
                      axis=0, keepdims=True)

    def fold(value):
        total = value[:, 0:128] * value[:, 0:128]
        for t in range(1, value.shape[1] // 128):
            total += value[:, 128 * t : 128 * t + 128] * value[:, 128 * t : 128 * t + 128]
        return jnp.sum(total, axis=0, keepdims=True)

    got(S.line_attn, r.r_attn)
    r.t_attn[0] = (r.r_attn[0].astype(F32) + r.r_attn[1].astype(F32)) + (
        r.r_attn[2].astype(F32) + r.r_attn[3].astype(F32)
    )
    trade(r.t_attn, r.f_attn, S.last_attn)
    got(S.line_qkv, r.r_qkv)
    r.t_qkv[...] = r.r_qkv[...].astype(F32)
    trade(r.t_qkv, r.f_qkv, S.last_qkv)
    got(S.late, r.late_got)
    over_group(r.late_got, r.late_all, S.late2)
    got(S.last_in, r.f_in.at[:, 0])
    got(S.last_attn, r.f_attn.at[:, 0])
    for h in range(2):
        for p in range(4):
            value = r.f_in[p, h]
            o_gin[:, 768 * p + 384 * h : 768 * p + 384 * h + 384] = value
            squares += fold(value)
        value = r.f_attn[0, h]
        o_gattn[:, 384 * h : 384 * h + 384] = value
        squares += fold(value)
    got(S.last_qkv, r.f_qkv.at[:, 0])
    where = {which: index for index, which in enumerate(HALVES) if which is not None}

    def packed_half(chunk, high):
        kind, rest = chunk // 12, chunk % 12
        index = where[(kind, rest % 3)]
        t = index // 2
        tile = r.f_qkv[rest // 3, t // 3, :, t % 3 * 128 : t % 3 * 128 + 128]
        return tile if index % 2 == high else pltpu.roll(tile, 64, 1)

    for t in range(18):
        o_gqkv[:, 128 * t : 128 * t + 128] = jnp.where(
            low, packed_half(2 * t, 0), packed_half(2 * t + 1, 1)
        )
    for p in range(4):
        for h in range(2):
            squares += fold(r.f_qkv[p, h])

    r.sq[me] = squares

    def send_sq(k):
        other = lax.rem(me + k, ALL)
        push(r.sq.at[me], r.sq.at[me], S.sq, lax.div(other, SEQ), lax.rem(other, SEQ))

    loop(ALL, send_sq, 1)
    sent(S.sq, r.sq.at[0:31])
    got(S.early2, r.early_all.at[0:3])
    got(S.late2, r.late_all.at[0:3])
    mods = []
    for k in range(4):
        early, late = r.early_all[k], r.late_all[k]
        rows = jnp.concatenate([late[1:3], early[1:5], jnp.zeros((2, 768), F32)], axis=0)
        o_dmod[k] = rows
        mods.append(rows)
    gain = jnp.concatenate(
        [
            sum(r.late_all[k][0:1] for k in range(4)),
            sum(r.early_all[k][0:1] for k in range(4)),
            (mods[0] + mods[1] + mods[2] + mods[3])[0:6],
        ],
        axis=0,
    )
    mask_row = sum(r.late_all[k][3:4] for k in range(4))
    o_gvec[0:8, :] = gain
    o_gvec[8:9, :] = mask_row
    o_gvec[9:16, :] = jnp.zeros((7, 768), F32)
    small = jnp.sum(gain * gain) + jnp.sum(mask_row * mask_row)
    conds = [r.conds_all[k][0:1].astype(BF).astype(F32) for k in range(4)]
    for k in range(4):
        for m in range(k, 4):
            term = jnp.sum(mods[k] * mods[m]) * jnp.sum(conds[k] * conds[m])
            small += term if m == k else 2.0 * term
    got(S.sq, r.sq.at[0:31])
    total = r.sq[0]
    for k in range(1, ALL):
        total += r.sq[k]
    o_norm[...] = jnp.broadcast_to(jnp.sqrt(jnp.sum(total) + small), (8, 128))

    for at, like in drains:
        left(at, like)


def run_layer(*args):
    shapes = (
        ((ROWS, WIDTH), F32),
        ((ROWS, WIDTH), F32),
        ((8, 128), F32),
        ((24, 3 * WIDTH), F32),
        ((24, WIDTH), F32),
        ((24, 4 * WIDTH), F32),
        ((96, WIDTH), F32),
        ((4, 8, WIDTH), F32),
        ((16, WIDTH), F32),
        ((8, 128), F32),
    )
    whole = pl.BlockSpec(memory_space=pltpu.VMEM)
    return pl.pallas_call(
        layer_kernel,
        out_shape=[jax.ShapeDtypeStruct(shape, kind) for shape, kind in shapes],
        in_specs=[whole] * len(args),
        out_specs=[whole] * len(shapes),
        scratch_shapes=[pltpu.VMEM(shape, kind) for shape, kind in SCRATCH.values()]
        + [pltpu.SemaphoreType.DMA((SEM_COUNT,)), pltpu.SemaphoreType.DMA((SEM_COUNT,))],
        compiler_params=pltpu.CompilerParams(
            collective_id=0, has_side_effects=True, vmem_limit_bytes=60 * 1024 * 1024
        ),
    )(*args)


def slices(
    tokens_in,
    cotangent,
    timesteps,
    span_start,
    span_len,
    vectors,
    w_ada,
    w_qkv,
    w_attn,
    w_in,
    w_out,
    m_vec,
    v_vec,
    m_ada,
    v_ada,
    m_qkv,
    v_qkv,
    m_attn,
    v_attn,
    m_in,
    v_in,
    m_out,
    v_out,
):
    place = lax.axis_index("seq")
    positions = place * ROWS + jnp.arange(ROWS, dtype=jnp.int32)
    masked = (positions >= span_start[0]) & (positions < span_start[0] + span_len[0])
    masked = masked[:, None]
    starts = (2 * jnp.arange(LINE, dtype=jnp.int32) + place % 2) * ROWS
    blocks = starts[:, None] + jnp.arange(ROWS, dtype=jnp.int32)[None, :]
    cosines, sines = rotary_tables(blocks.reshape(-1))
    none = jnp.zeros_like(sines)
    turn = jnp.stack(
        [
            jnp.concatenate([cosines] * 4, axis=1),
            jnp.concatenate([-sines, none] * 2, axis=1),
            jnp.concatenate([none, sines] * 2, axis=1),
        ]
    ).reshape(3, LINE, ROWS, 128)
    cond = jnp.broadcast_to(cond_input(timesteps), (8, COND))
    y, dx0, norm, g_qkv, g_attn, g_in, g_out, dmod, g_vec, conds = run_layer(
        tokens_in[0],
        cotangent[0],
        cond,
        jnp.broadcast_to(masked.astype(F32), (ROWS, 128)),
        vectors,
        jnp.pad(w_ada.astype(BF), ((0, 0), (0, 384 - w_ada.shape[1]))),
        w_qkv,
        w_attn,
        w_in,
        w_out,
        turn,
    )
    block_out = y.astype(BF)[None]
    grad_input = jnp.where(masked, 0.0, dx0)[None]
    grad_norm = norm[0, 0]
    clip_factor = jnp.minimum(1.0, CLIP / (grad_norm + 1e-06))
    rank = lax.axis_index(("dp", "seq"))
    wide, narrow = w_ada.shape[1], m_vec.shape[1]
    own_mod = lax.dynamic_slice_in_dim(
        dmod[:, 0:6].reshape(4, 6 * WIDTH), rank * wide, wide, 1
    )
    g_ada = jnp.dot(
        conds[0:4].astype(BF).astype(F32).T, own_mod, precision=lax.Precision.HIGHEST
    )
    g_vec = lax.dynamic_slice_in_dim(g_vec[0:9], rank * narrow, narrow, 1)
    own_vectors = lax.dynamic_slice_in_dim(vectors, rank * narrow, narrow, 1)
    vec_out = adam_step(own_vectors, g_vec * clip_factor, m_vec, v_vec, RATE_VECTORS, 0.0)
    ada_out = adam_step(w_ada, g_ada * clip_factor, m_ada, v_ada, RATE, DECAY)
    qkv_out = adam_step(w_qkv, g_qkv * clip_factor, m_qkv, v_qkv, RATE, DECAY)
    attn_out = adam_step(w_attn, g_attn * clip_factor, m_attn, v_attn, RATE, DECAY)
    in_out = adam_step(w_in, g_in * clip_factor, m_in, v_in, RATE, DECAY)
    out_out = adam_step(w_out, g_out * clip_factor, m_out, v_out, RATE, DECAY)
    return (
        block_out,
        grad_input,
        grad_norm,
        *vec_out,
        *ada_out,
        *qkv_out,
        *attn_out,
        *in_out,
        *out_out,
    )


def solution(mesh):
    in_specs = (
        P("dp", "seq", None),
        P("dp", "seq", None),
        P("dp"),
        P("dp"),
        P("dp"),
        P(),
        P(None, ("dp", "seq")),
        P(("dp", "seq"), None),
        P(("dp", "seq"), None),
        P(("dp", "seq"), None),
        P(("dp", "seq"), None),
        P(None, ("dp", "seq")),
        P(None, ("dp", "seq")),
        P(None, ("dp", "seq")),
        P(None, ("dp", "seq")),
        P(("dp", "seq"), None),
        P(("dp", "seq"), None),
        P(("dp", "seq"), None),
        P(("dp", "seq"), None),
        P(("dp", "seq"), None),
        P(("dp", "seq"), None),
        P(("dp", "seq"), None),
        P(("dp", "seq"), None),
    )
    out_specs = (
        P("dp", "seq", None),
        P("dp", "seq", None),
        P(),
        P(None, ("dp", "seq")),
        P(None, ("dp", "seq")),
        P(None, ("dp", "seq")),
        P(None, ("dp", "seq")),
        P(None, ("dp", "seq")),
        P(None, ("dp", "seq")),
        P(("dp", "seq"), None),
        P(("dp", "seq"), None),
        P(("dp", "seq"), None),
        P(("dp", "seq"), None),
        P(("dp", "seq"), None),
        P(("dp", "seq"), None),
        P(("dp", "seq"), None),
        P(("dp", "seq"), None),
        P(("dp", "seq"), None),
        P(("dp", "seq"), None),
        P(("dp", "seq"), None),
        P(("dp", "seq"), None),
    )
    sizes = dict(mesh.shape)
    local = slices if (sizes["dp"], sizes["seq"]) == (4, 8) else plain
    return jax.shard_map(local, mesh=mesh, in_specs=in_specs, out_specs=out_specs, check_vma=False)
```

```python
from functools import partial
import math
from types import SimpleNamespace

import jax
import jax.numpy as jnp
from jax import lax
from jax.experimental import pallas as pl
from jax.experimental.pallas import tpu as pltpu
from jax.sharding import PartitionSpec as P

HD = 64
COND = 128
STEP = 10


BETA_ONE = 0.9
BETA_TWO = 0.999
ADAM_EPS = 1e-08
RATE = 0.1
RATE_VECTORS = 0.3
DECAY = 0.01
CLIP = 1.0
NORM_EPS = 1e-05


def cond_input(timesteps):
    half_cond = COND // 2
    freqs = jnp.exp(jnp.arange(half_cond, dtype=jnp.float32) * (-math.log(10000.0) / half_cond))
    angles = timesteps.astype(jnp.float32)[:, None] * freqs[None, :]
    return jax.nn.silu(jnp.concatenate([jnp.cos(angles), jnp.sin(angles)], axis=1))


def rotary_tables(positions):
    half_head = HD // 2
    inverse = jnp.exp(jnp.arange(half_head, dtype=jnp.float32) * (-math.log(10000.0) / half_head))
    angles = positions.astype(jnp.float32)[:, None] * inverse[None, :]
    return (jnp.cos(angles), jnp.sin(angles))


def rotate(values, cosines, sines):
    half_head = values.shape[-1] // 2
    first = values[..., :half_head]
    second = values[..., half_head:]
    cos_b = cosines[:, None, :]
    sin_b = sines[:, None, :]
    return jnp.concatenate(
        [first * cos_b - second * sin_b, second * cos_b + first * sin_b], axis=-1
    )


def rotate_back(grads, cosines, sines):
    half_head = grads.shape[-1] // 2
    first = grads[..., :half_head]
    second = grads[..., half_head:]
    cos_b = cosines[:, None, :]
    sin_b = sines[:, None, :]
    return jnp.concatenate(
        [first * cos_b + second * sin_b, second * cos_b - first * sin_b], axis=-1
    )


def normalize(values):
    centre = jnp.mean(values, axis=-1, keepdims=True)
    centred = values - centre
    inverse = lax.rsqrt(jnp.mean(centred * centred, axis=-1, keepdims=True) + NORM_EPS)
    return (centred * inverse, inverse)


def norm_back(normed, inverse, grad):
    return inverse * (
        grad
        - jnp.mean(grad, axis=-1, keepdims=True)
        - normed * jnp.mean(grad * normed, axis=-1, keepdims=True)
    )


def split_kv(block, width):
    seqs, block_rows = (block.shape[0], block.shape[1])
    keys = block[..., :width].reshape(seqs, block_rows, width // HD, HD)
    values = block[..., width:].reshape(seqs, block_rows, width // HD, HD)
    return (keys, values)


def attend_piece(carry, piece, queries, width, factor):
    piece_rows = piece.shape[1]
    size = math.gcd(piece_rows, 512)

    def attend_one_block(index, state):
        running, denom, accum = state
        block = lax.dynamic_slice_in_dim(piece, index * size, size, 1)
        keys, values = split_kv(block, width)
        scores = (
            jnp.einsum("sqhd,skhd->shqk", queries, keys, preferred_element_type=jnp.float32)
            * factor
        )
        highest = jnp.maximum(running, jnp.max(scores, axis=-1))
        shrink = jnp.exp(running - highest)
        weights = jnp.exp(scores - highest[..., None])
        denom = denom * shrink + jnp.sum(weights, axis=-1)
        accum = accum * shrink[..., None] + jnp.einsum(
            "shqk,skhd->shqd",
            weights.astype(jnp.bfloat16),
            values,
            preferred_element_type=jnp.float32,
        )
        return (highest, denom, accum)

    return lax.fori_loop(0, piece_rows // size, attend_one_block, carry)


def block_grads(block, queries, grad_out, logsum, delta, width, factor):
    keys, values = split_kv(block, width)
    scores = (
        jnp.einsum("sqhd,skhd->shqk", queries, keys, preferred_element_type=jnp.float32) * factor
    )
    probs = jnp.exp(scores - logsum[..., None])
    dprobs = jnp.einsum("sqhd,skhd->shqk", grad_out, values, preferred_element_type=jnp.float32)
    dscores = (probs * (dprobs - delta[..., None])).astype(jnp.bfloat16)
    return (keys, probs, dscores)


def query_grads(kv_all, queries, grad_out, logsum, delta, width, factor):
    total_rows = kv_all.shape[1]
    size = math.gcd(total_rows, 512)

    def query_one_block(index, accum):
        block = lax.dynamic_slice_in_dim(kv_all, index * size, size, 1)
        keys, probs, dscores = block_grads(block, queries, grad_out, logsum, delta, width, factor)
        return accum + factor * jnp.einsum(
            "shqk,skhd->sqhd", dscores, keys, preferred_element_type=jnp.float32
        )

    return lax.fori_loop(
        0, total_rows // size, query_one_block, jnp.zeros(queries.shape, jnp.float32)
    )


def key_grads(kv_all, queries, grad_out, logsum, delta, width, factor, count):
    size = math.gcd(count, 512)
    seqs = queries.shape[0]

    def key_one_block(index, accum):
        block = lax.dynamic_slice_in_dim(kv_all, index * size, size, 1)
        keys, probs, dscores = block_grads(block, queries, grad_out, logsum, delta, width, factor)
        grad_vals = jnp.einsum(
            "shqk,sqhd->skhd",
            probs.astype(jnp.bfloat16),
            grad_out,
            preferred_element_type=jnp.float32,
        )
        grad_keys = factor * jnp.einsum(
            "shqk,sqhd->skhd", dscores, queries, preferred_element_type=jnp.float32
        )
        joined = jnp.concatenate(
            [grad_keys.reshape(seqs, size, width), grad_vals.reshape(seqs, size, width)], axis=-1
        )
        return lax.dynamic_update_slice_in_dim(
            accum, jnp.transpose(joined, (1, 0, 2)), index * size, 0
        )

    initial = jnp.zeros((count, seqs, 2 * width), jnp.float32)
    return lax.fori_loop(0, count // size, key_one_block, initial)


def adam_step(weight, grad, first, second, rate, decay_rate):
    new_first = BETA_ONE * first + (1.0 - BETA_ONE) * grad
    new_second = BETA_TWO * second + (1.0 - BETA_TWO) * grad * grad
    fixed_first = new_first / (1.0 - BETA_ONE**STEP)
    fixed_second = new_second / (1.0 - BETA_TWO**STEP)
    new_weight = weight - rate * (
        fixed_first / (jnp.sqrt(fixed_second) + ADAM_EPS) + decay_rate * weight
    )
    return (new_first, new_second, new_weight)


def mod_back(grad_hidden, ln_values, normed, scale_part, gain):
    grad_shift = jnp.sum(grad_hidden, axis=1)
    grad_scale = jnp.sum(grad_hidden * ln_values, axis=1)
    grad_ln = grad_hidden * (1.0 + scale_part)
    grad_gain = jnp.sum(grad_ln * normed, axis=(0, 1))
    return (grad_shift, grad_scale, grad_gain, grad_ln * gain)


def plain(
    tokens_in,
    cotangent,
    timesteps,
    span_start,
    span_len,
    vectors,
    w_ada,
    w_qkv,
    w_attn,
    w_in,
    w_out,
    m_vec,
    v_vec,
    m_ada,
    v_ada,
    m_qkv,
    v_qkv,
    m_attn,
    v_attn,
    m_in,
    v_in,
    m_out,
    v_out,
):
    seqs, group, width = tokens_in.shape
    heads = width // HD
    factor = HD ** (-0.5)
    flat_rows = seqs * group
    full_ada, full_qkv, full_attn, full_in, full_out = (
        lax.all_gather(w_ada.astype(jnp.bfloat16), ("dp", "seq"), axis=1, tiled=True),
        lax.all_gather(w_qkv.astype(jnp.bfloat16), ("dp", "seq"), axis=0, tiled=True),
        lax.all_gather(w_attn.astype(jnp.bfloat16), ("dp", "seq"), axis=0, tiled=True),
        lax.all_gather(w_in.astype(jnp.bfloat16), ("dp", "seq"), axis=0, tiled=True),
        lax.all_gather(w_out.astype(jnp.bfloat16), ("dp", "seq"), axis=0, tiled=True),
    )
    positions = lax.axis_index("seq") * group + jnp.arange(group, dtype=jnp.int32)
    masked = (positions[None, :] >= span_start[:, None]) & (
        positions[None, :] < (span_start + span_len)[:, None]
    )
    cond_bf = cond_input(timesteps).astype(jnp.bfloat16)
    modulation = jnp.dot(cond_bf, full_ada, preferred_element_type=jnp.float32) + vectors[
        2:8
    ].reshape(1, 6 * width)
    pieces = [modulation[:, which * width : (which + 1) * width][:, None, :] for which in range(6)]
    shift_one, scale_one, gate_one, shift_two, scale_two, gate_two = pieces
    start_tokens = jnp.where(
        masked[..., None], vectors[8][None, None, :], tokens_in.astype(jnp.float32)
    )
    normed_one, inv_one = normalize(start_tokens)
    ln_one = normed_one * vectors[0]
    hidden_one = (
        (ln_one * (1.0 + scale_one) + shift_one).astype(jnp.bfloat16).reshape(flat_rows, width)
    )
    projected = jnp.dot(hidden_one, full_qkv, preferred_element_type=jnp.float32).reshape(
        seqs, group, 3 * width
    )
    cosines, sines = rotary_tables(positions)
    queries = rotate(projected[..., :width].reshape(seqs, group, heads, HD), cosines, sines).astype(
        jnp.bfloat16
    )
    keys_here = rotate(
        projected[..., width : 2 * width].reshape(seqs, group, heads, HD), cosines, sines
    ).astype(jnp.bfloat16)
    values_here = projected[..., 2 * width :].astype(jnp.bfloat16)
    kv_local = jnp.concatenate([keys_here.reshape(seqs, group, width), values_here], axis=-1)
    initial = (
        jnp.full((seqs, heads, group), -1e30, jnp.float32),
        jnp.zeros((seqs, heads, group), jnp.float32),
        jnp.zeros((seqs, heads, group, HD), jnp.float32),
    )
    running, denom, accum = attend_piece(
        initial, lax.all_gather(kv_local, "seq", axis=1, tiled=True), queries, width, factor
    )
    attn_heads = accum / denom[..., None]
    logsum = running + jnp.log(denom)
    attn_rows = jnp.transpose(attn_heads, (0, 2, 1, 3)).reshape(flat_rows, width)
    attn_bf = attn_rows.astype(jnp.bfloat16)
    branch_one = jnp.dot(attn_bf, full_attn, preferred_element_type=jnp.float32).reshape(
        seqs, group, width
    )
    mid_tokens = start_tokens + gate_one * branch_one
    normed_two, inv_two = normalize(mid_tokens)
    ln_two = normed_two * vectors[1]
    hidden_two = (
        (ln_two * (1.0 + scale_two) + shift_two).astype(jnp.bfloat16).reshape(flat_rows, width)
    )
    pre_act = jnp.dot(hidden_two, full_in, preferred_element_type=jnp.float32)
    activ, gelu_back = jax.vjp(partial(jax.nn.gelu, approximate=True), pre_act)
    activ_bf = activ.astype(jnp.bfloat16)
    branch_two = jnp.dot(activ_bf, full_out, preferred_element_type=jnp.float32).reshape(
        seqs, group, width
    )
    block_out = (mid_tokens + gate_two * branch_two).astype(jnp.bfloat16)
    grad_y = cotangent.astype(jnp.float32)
    grad_gate_two = jnp.sum(grad_y * branch_two, axis=1)
    grad_branch_two = (grad_y * gate_two).astype(jnp.bfloat16).reshape(flat_rows, width)
    grad_w_out = jnp.dot(activ_bf.T, grad_branch_two, preferred_element_type=jnp.float32)
    grad_activ = jnp.dot(grad_branch_two, full_out.T, preferred_element_type=jnp.float32)
    grad_pre = gelu_back(grad_activ)[0].astype(jnp.bfloat16)
    grad_w_in = jnp.dot(hidden_two.T, grad_pre, preferred_element_type=jnp.float32)
    grad_hidden_two = jnp.dot(grad_pre, full_in.T, preferred_element_type=jnp.float32).reshape(
        seqs, group, width
    )
    grad_shift_two, grad_scale_two, grad_gain_two, grad_normed_two = mod_back(
        grad_hidden_two, ln_two, normed_two, scale_two, vectors[1]
    )
    grad_mid = grad_y + norm_back(normed_two, inv_two, grad_normed_two)
    grad_gate_one = jnp.sum(grad_mid * branch_one, axis=1)
    grad_branch_one = (grad_mid * gate_one).astype(jnp.bfloat16).reshape(flat_rows, width)
    grad_w_attn = jnp.dot(attn_bf.T, grad_branch_one, preferred_element_type=jnp.float32)
    grad_attn_bf = (
        jnp.dot(grad_branch_one, full_attn.T, preferred_element_type=jnp.float32)
        .astype(jnp.bfloat16)
        .reshape(seqs, group, heads, HD)
    )
    delta = jnp.einsum("sqhd,shqd->shq", grad_attn_bf.astype(jnp.float32), attn_heads)
    kv_all = lax.all_gather(kv_local, "seq", axis=1, tiled=True)
    grad_queries = query_grads(kv_all, queries, grad_attn_bf, logsum, delta, width, factor)
    grad_kv = jnp.transpose(
        lax.psum_scatter(
            key_grads(
                kv_all,
                queries,
                grad_attn_bf,
                logsum,
                delta,
                width,
                factor,
                group * lax.axis_size("seq"),
            ).astype(jnp.bfloat16),
            "seq",
            scatter_dimension=0,
            tiled=True,
        ).astype(jnp.float32),
        (1, 0, 2),
    )
    grad_keys = grad_kv[..., :width].reshape(seqs, group, heads, HD)
    grad_qkv = jnp.concatenate(
        [
            rotate_back(grad_queries, cosines, sines).reshape(seqs, group, width),
            rotate_back(grad_keys, cosines, sines).reshape(seqs, group, width),
            grad_kv[..., width:],
        ],
        axis=-1,
    )
    grad_qkv = grad_qkv.astype(jnp.bfloat16).reshape(flat_rows, 3 * width)
    grad_w_qkv = jnp.dot(hidden_one.T, grad_qkv, preferred_element_type=jnp.float32)
    grad_hidden_one = jnp.dot(grad_qkv, full_qkv.T, preferred_element_type=jnp.float32).reshape(
        seqs, group, width
    )
    grad_shift_one, grad_scale_one, grad_gain_one, grad_normed_one = mod_back(
        grad_hidden_one, ln_one, normed_one, scale_one, vectors[0]
    )
    grad_start = grad_mid + norm_back(normed_one, inv_one, grad_normed_one)
    grad_mask_row = jnp.sum(jnp.where(masked[..., None], grad_start, 0.0), axis=(0, 1))
    grad_input = jnp.where(masked[..., None], 0.0, grad_start)
    grad_mod = jnp.concatenate(
        [
            grad_shift_one,
            grad_scale_one,
            grad_gate_one,
            grad_shift_two,
            grad_scale_two,
            grad_gate_two,
        ],
        axis=1,
    )
    grad_w_ada = jnp.dot(cond_bf.astype(jnp.float32).T, grad_mod, precision=lax.Precision.HIGHEST)
    grad_vectors = jnp.concatenate(
        [
            grad_gain_one[None, :],
            grad_gain_two[None, :],
            jnp.sum(grad_mod, axis=0).reshape(6, width),
            grad_mask_row[None, :],
        ],
        axis=0,
    )
    red_ada, red_qkv, red_attn, red_in, red_out, red_vec = (
        lax.psum_scatter(grad_w_ada, ("dp", "seq"), scatter_dimension=1, tiled=True),
        lax.psum_scatter(grad_w_qkv, ("dp", "seq"), scatter_dimension=0, tiled=True),
        lax.psum_scatter(grad_w_attn, ("dp", "seq"), scatter_dimension=0, tiled=True),
        lax.psum_scatter(grad_w_in, ("dp", "seq"), scatter_dimension=0, tiled=True),
        lax.psum_scatter(grad_w_out, ("dp", "seq"), scatter_dimension=0, tiled=True),
        lax.psum_scatter(grad_vectors, ("dp", "seq"), scatter_dimension=1, tiled=True),
    )
    local_squares = jnp.float32(0.0)
    for reduced in (red_vec, red_ada, red_qkv, red_attn, red_in, red_out):
        local_squares = local_squares + jnp.sum(reduced * reduced)
    grad_norm = jnp.sqrt(lax.psum(local_squares, ("dp", "seq")))
    clip_factor = jnp.minimum(1.0, CLIP / (grad_norm + 1e-06))
    columns = red_vec.shape[1]
    own_vectors = lax.dynamic_slice_in_dim(
        vectors, lax.axis_index(("dp", "seq")) * columns, columns, 1
    )
    vec_out = adam_step(own_vectors, red_vec * clip_factor, m_vec, v_vec, RATE_VECTORS, 0.0)
    ada_out = adam_step(w_ada, red_ada * clip_factor, m_ada, v_ada, RATE, DECAY)
    qkv_out = adam_step(w_qkv, red_qkv * clip_factor, m_qkv, v_qkv, RATE, DECAY)
    attn_out = adam_step(w_attn, red_attn * clip_factor, m_attn, v_attn, RATE, DECAY)
    in_out = adam_step(w_in, red_in * clip_factor, m_in, v_in, RATE, DECAY)
    out_out = adam_step(w_out, red_out * clip_factor, m_out, v_out, RATE, DECAY)
    return (
        block_out,
        grad_input,
        grad_norm,
        vec_out[0],
        vec_out[1],
        vec_out[2],
        ada_out[0],
        ada_out[1],
        ada_out[2],
        qkv_out[0],
        qkv_out[1],
        qkv_out[2],
        attn_out[0],
        attn_out[1],
        attn_out[2],
        in_out[0],
        in_out[1],
        in_out[2],
        out_out[0],
        out_out[1],
        out_out[2],
    )


F32, BF = jnp.float32, jnp.bfloat16
MESH = pl.DeviceIdType.MESH
DP, LINE, SEQ, CHIPS, ALL = 4, 4, 8, 16, 32
ROWS, WIDTH, PACK = 128, 768, 640
HALF = WIDTH // 2
HALVES = ((0, 0), (0, 1), (0, 2), (2, 2), (1, 0), (1, 1), (1, 2), None, (2, 0), (2, 1))

def numbered(**counts):
    at = {}
    for name, count in counts.items():
        at[name] = sum(counts[other] for other in at)
    return SimpleNamespace(**at), sum(counts.values())


S, SEM_COUNT = numbered(
    cond=1,
    mix_qkv=1,
    mix_in=1,
    mix_attn=1,
    mod=1,
    w_qkv=1,
    w_attn=1,
    w_in=1,
    w_out=1,
    group_qkv=1,
    group_attn=1,
    fw_qkv=1,
    fw_attn=1,
    fw_in=1,
    fw_out=1,
    h1=4,
    h2=4,
    dm=4,
    xf=4,
    o=1,
    mm=1,
    dh2=1,
    do=1,
    gp=1,
    dh1=1,
    pair_out=1,
    pair_in=1,
    pair_attn=1,
    pair_qkv=1,
    plane_attn=1,
    plane_qkv=1,
    line_out=1,
    line_in=1,
    line_attn=1,
    line_qkv=1,
    last_in=1,
    last_attn=1,
    last_qkv=1,
    early=1,
    early2=1,
    late=1,
    late2=1,
    sq=1,
)

SCRATCH = dict(
    wide_qkv=((48, 3072), F32),
    wide_in=((48, 3072), F32),
    wide_attn=((48, 768), F32),
    s_qkv=((48, 3072), BF),
    s_in=((48, 3072), BF),
    s_attn=((48, 768), BF),
    s_out=((96, 768), BF),
    w_qkv=((768, 768), BF),
    w_in=((768, 768), BF),
    w_attn=((768, 768), BF),
    w_out=((4, 2, 96, 768), BF),
    conds_all=((4, 8, 128), F32),
    mod_send=((4, 4, 128), F32),
    mod_got=((32, 4, 128), F32),
    mod_flat=((40, 128), F32),
    mod_pad=((8, 384), F32),
    turn=((2, 4, 128, 128), F32),
    dmod_flat=((4, 40, 128), F32),
    mod=((8, 768), F32),
    x0=((128, 768), F32),
    n1=((128, 768), F32),
    inv1=((128, 128), F32),
    x1=((128, 768), F32),
    n2=((128, 768), F32),
    inv2=((128, 128), F32),
    a=((128, 768), F32),
    dx1=((128, 768), F32),
    h1=((4, 128, 768), BF),
    h2=((4, 128, 768), BF),
    dm=((4, 128, 768), BF),
    gb=((4, 128, 768), BF),
    du=((4, 128, 768), BF),
    xb=((2, 4, 128, 640), BF),
    pt=((3, 1024, 512), BF),
    ot=((2, 128, 512), F32),
    os=((4, 128, 256), BF),
    ob=((4, 128, 256), BF),
    mms=((4, 128, 768), BF),
    mmr=((4, 128, 768), BF),
    dhs=((4, 128, 768), BF),
    dhr=((4, 128, 768), BF),
    das=((128, 768), BF),
    dos=((4, 128, 256), BF),
    dob=((4, 128, 256), BF),
    dst=((1024, 512), BF),
    ga=((1024, 640), F32),
    gps=((512, 512), BF),
    gpr=((512, 512), BF),
    dqkv=((4, 128, 768), BF),
    d1s=((4, 128, 768), BF),
    d1r=((4, 128, 768), BF),
    g_out=((4, 2, 96, 768), BF),
    g_in=((2, 768, 384), BF),
    g_attn=((2, 768, 384), BF),
    g_qkv=((2, 768, 384), BF),
    p_out=((4, 96, 768), BF),
    p_in=((768, 384), BF),
    p_attn=((768, 384), BF),
    p_qkv=((768, 384), BF),
    q_attn=((4, 192, 384), BF),
    q_qkv=((4, 192, 384), BF),
    m_attn=((192, 384), BF),
    m_qkv=((192, 384), BF),
    r_out=((4, 96, 768), BF),
    r_in=((16, 48, 384), BF),
    r_attn=((4, 48, 384), BF),
    r_qkv=((4, 48, 384), BF),
    t_in=((4, 48, 384), F32),
    t_attn=((1, 48, 384), F32),
    t_qkv=((4, 48, 384), F32),
    f_in=((4, 2, 24, 384), F32),
    f_attn=((1, 2, 24, 384), F32),
    f_qkv=((4, 2, 24, 384), F32),
    early=((8, 768), F32),
    early_got=((8, 8, 768), F32),
    early_all=((4, 8, 768), F32),
    late=((4, 768), F32),
    late_got=((8, 4, 768), F32),
    late_all=((4, 4, 768), F32),
    sq=((32, 1, 128), F32),
)


def dot(left, right):
    return jnp.dot(left, right, preferred_element_type=F32)


def dot_nt(left, right):
    return lax.dot_general(left, right, (((1,), (1,)), ((), ())), preferred_element_type=F32)


def dot_tn(left, right):
    return lax.dot_general(left, right, (((0,), (0,)), ((), ())), preferred_element_type=F32)


def loop(count, body, start=0):
    def step(index, carry):
        body(index)
        return carry

    lax.fori_loop(start, count, step, 0)


def layer_kernel(
    i_time,
    i_start,
    i_len,
    i_tok,
    i_cot,
    i_vec,
    i_wada,
    i_wqkv,
    i_wattn,
    i_win,
    i_wout,
    o_y,
    o_dx,
    o_norm,
    o_gqkv,
    o_gattn,
    o_gin,
    o_gout,
    o_dmod,
    o_gvec,
    o_vec,
    o_conds,
    *scratch,
):
    r = SimpleNamespace(**dict(zip(SCRATCH, scratch)))
    send_sems, recv_sems = scratch[-2:]
    b, s = lax.axis_index("dp"), lax.axis_index("seq")
    z, c = lax.div(s, 2), lax.rem(s, 2)
    mate = s + 1 - 2 * c
    chip = b * LINE + z
    me = b * SEQ + s
    drains = []

    def push(src, dst, at, to_b, to_s):
        pltpu.make_async_remote_copy(
            src_ref=src,
            dst_ref=dst,
            send_sem=send_sems.at[at],
            recv_sem=recv_sems.at[at],
            device_id=(to_b, to_s),
            device_id_type=MESH,
        ).start()

    def keep(src, dst, at):
        pltpu.make_async_copy(src, dst, recv_sems.at[at]).start()

    def got(at, like):
        pltpu.make_async_copy(like, like, recv_sems.at[at]).wait()

    def left(at, like):
        pltpu.make_async_copy(like, like, send_sems.at[at]).wait()

    def sent(at, like):
        drains.append((at, like))

    def peers(body):
        for k in (1, 2, 3):
            body(lax.rem(b + k, DP))

    def stack(body):
        for k in (1, 2, 3):
            body(lax.rem(z + k, LINE))

    lane = lax.broadcasted_iota(jnp.int32, (1, 128), 1)
    low = lane < 64
    own24 = pl.ds(pl.multiple_of(24 * c, 8), 24)
    mate24 = pl.ds(pl.multiple_of(24 * (1 - c), 8), 24)
    part = pl.ds(pl.multiple_of(HALF * c, 128), HALF)
    chip_rows = pl.ds(pl.multiple_of(48 * chip, 16), 48)
    group_rows = pl.ds(pl.multiple_of(192 * b, 16), 192)

    barrier = pltpu.get_barrier_semaphore()

    def greet(k):
        other = lax.rem(me + k, ALL)
        pl.semaphore_signal(
            barrier, inc=1, device_id=(lax.div(other, SEQ), lax.rem(other, SEQ)), device_id_type=MESH
        )

    loop(ALL, greet, 1)

    def natural(kind, p, head):
        return kind * WIDTH + 192 * p + 64 * head

    def half_at(ref, column, high):
        tile = ref[:, column // 128 * 128 : column // 128 * 128 + 128]
        return tile if (column % 128 == 64) == high else pltpu.roll(tile, 64, 1)

    for p in range(4):
        for tile in range(5):
            pair = []
            for high in (0, 1):
                which = HALVES[2 * tile + high]
                pair.append(
                    jnp.zeros((24, 128), F32)
                    if which is None
                    else half_at(i_wqkv, natural(which[0], p, which[1]), bool(high))
                )
            r.wide_qkv[own24, 768 * p + 128 * tile : 768 * p + 128 * tile + 128] = jnp.where(
                low, pair[0], pair[1]
            )
        r.wide_qkv[own24, 768 * p + 640 : 768 * p + 768] = jnp.zeros((24, 128), F32)
    r.wide_in[own24, :] = i_win[...]
    r.wide_attn[own24, :] = i_wattn[...]
    r.s_out[...] = i_wout[...].astype(BF)
    lanes8 = lax.broadcasted_iota(jnp.int32, (8, 128), 1)
    half_cond = COND // 2
    speed = jnp.exp((lanes8 % half_cond).astype(F32) * (-math.log(10000.0) / half_cond))
    angle = i_time[0].astype(F32) * speed
    wave = jnp.where(lanes8 < half_cond, jnp.cos(angle), jnp.sin(angle))
    r.conds_all[b] = wave * (1.0 / (1.0 + jnp.exp(-wave)))
    pl.semaphore_wait(barrier, ALL - 1)

    def stack_rows(to):
        push(r.s_out, r.w_out.at[z, c], S.w_out, b, 2 * to + c)

    peers(lambda to: push(r.conds_all.at[b], r.conds_all.at[b], S.cond, to, s))
    sent(S.cond, r.conds_all.at[0:3])
    push(r.wide_qkv.at[own24], r.wide_qkv.at[own24], S.mix_qkv, b, mate)
    sent(S.mix_qkv, r.wide_qkv.at[0:24])
    push(r.wide_attn.at[own24], r.wide_attn.at[own24], S.mix_attn, b, mate)
    sent(S.mix_attn, r.wide_attn.at[0:24])
    push(r.wide_in.at[own24], r.wide_in.at[own24], S.mix_in, b, mate)
    sent(S.mix_in, r.wide_in.at[0:24])
    stack(stack_rows)
    keep(r.s_out, r.w_out.at[z, c], S.w_out)
    sent(S.w_out, r.w_out.at[0:3, 0])

    got(S.cond, r.conds_all.at[0:3])
    row8 = lax.broadcasted_iota(jnp.int32, (8, 128), 0)
    cond4 = jnp.zeros((8, 128), F32)
    for k in range(4):
        cond4 = jnp.where(row8 == k, r.conds_all[k], cond4)
    o_conds[...] = cond4
    wide = i_wada.shape[1]
    r.mod_pad[...] = jnp.zeros((8, 384), F32)
    r.mod_pad[:, 0:wide] = dot(cond4.astype(BF), i_wada[...].astype(BF))
    columns = pltpu.roll(r.mod_pad[...], lax.rem(wide * me, 128), 1)
    for k in range(4):
        for t in range(3):
            r.mod_send[k, t : t + 1, :] = columns[k : k + 1, 128 * t : 128 * t + 128]
        r.mod_send[k, 3:4, :] = jnp.zeros((1, 128), F32)

    def send_mod(k):
        other = lax.rem(me + k, ALL)
        ob = lax.div(other, SEQ)
        push(r.mod_send.at[ob], r.mod_got.at[me], S.mod, ob, lax.rem(other, SEQ))

    loop(ALL, send_mod, 1)
    sent(S.mod, r.mod_got.at[0:31])
    keep(r.mod_send.at[b], r.mod_got.at[me], S.mod)

    def block(src, first):
        return src.at[:, pl.ds(pl.multiple_of(first, 128), HALF)]

    def spread(src, dst, at):
        def one(k):
            to = lax.rem(chip + k, CHIPS)
            to_b, to_z = lax.div(to, LINE), lax.rem(to, LINE)
            push(
                block(src, WIDTH * to_b + HALF * c),
                dst.at[chip_rows, part],
                at,
                to_b,
                2 * to_z + c,
            )

        loop(CHIPS, one, 1)
        keep(block(src, WIDTH * b + HALF * c), dst.at[chip_rows, part], at)
        sent(at, dst.at[0:720, 0:HALF])

    def along_line(src, dst, at, step):
        stack(
            lambda to: push(
                block(src, step * to + HALF * c), dst.at[chip_rows, part], at, b, 2 * to + c
            )
        )
        keep(block(src, step * z + HALF * c), dst.at[chip_rows, part], at)
        sent(at, dst.at[0:144, 0:HALF])

    def over_plane(dst, first, at):
        got(first, dst.at[0:192, 0:HALF])
        peers(
            lambda to: push(dst.at[group_rows, part], dst.at[group_rows, part], at, to, s)
        )
        sent(at, dst.at[0:576, 0:HALF])

    def share(dst, at, onward, rows):
        got(at, dst.at[0:rows, 0:HALF])
        push(dst.at[:, part], dst.at[:, part], onward, b, mate)
        sent(onward, dst.at[:, 0:HALF])

    got(S.mix_qkv, r.wide_qkv.at[0:24])
    r.s_qkv[...] = r.wide_qkv[...].astype(BF)
    along_line(r.s_qkv, r.w_qkv, S.w_qkv, WIDTH)
    got(S.mix_attn, r.wide_attn.at[0:24])
    r.s_attn[...] = r.wide_attn[...].astype(BF)
    along_line(r.s_attn, r.w_attn, S.w_attn, 0)

    place = s * ROWS + lax.broadcasted_iota(jnp.int32, (ROWS, 1), 0)
    hidden = (place >= i_start[0]) & (place < i_start[0] + i_len[0])
    x0 = jnp.where(hidden, i_vec[8:9, :], i_tok[0].astype(F32))
    r.x0[...] = x0
    n1, inv1 = normalize(x0)
    r.n1[...] = n1
    r.inv1[...] = jnp.broadcast_to(inv1, (ROWS, 128))

    lanes = lax.broadcasted_iota(jnp.int32, (ROWS, 128), 1)
    first_half = lanes % HD < HD // 2
    speed = jnp.exp((lanes % (HD // 2)).astype(F32) * (-math.log(10000.0) / (HD // 2)))
    row = lax.broadcasted_iota(jnp.int32, (ROWS, 128), 0)

    def table(k):
        angle = ((2 * k + c) * ROWS + row).astype(F32) * speed
        r.turn[0, k] = jnp.cos(angle)
        sine = jnp.sin(angle)
        r.turn[1, k] = jnp.where(first_half, -sine, sine)

    loop(LINE, table)

    got(S.mod, r.mod_got)
    r.mod_flat[...] = jnp.zeros((40, 128), F32)
    for k in range(ALL):
        first = 9 * k // 8
        r.mod_flat[first : first + 3, :] += r.mod_got[k, 0:3, :]
    for k in range(6):
        row = jnp.concatenate(
            [r.mod_flat[6 * k + t : 6 * k + t + 1, :] for t in range(6)], axis=1
        )
        r.mod[k : k + 1, :] = row + i_vec[2 + k : 3 + k, :]

    def mod(k):
        return r.mod[k : k + 1, :]

    def vec(k):
        return i_vec[k : k + 1, :]

    r.h1[z] = (r.n1[...] * vec(0) * (1.0 + mod(1)) + mod(0)).astype(BF)
    stack(lambda to: push(r.h1.at[z], r.h1.at[z], S.h1 + z, b, 2 * to + c))
    sent(S.h1 + z, r.h1.at[0:3])
    r.dm[b] = (i_cot[0].astype(F32) * mod(5)).astype(BF)
    over_plane(r.w_qkv, S.w_qkv, S.group_qkv)
    got(S.mix_in, r.wide_in.at[0:24])
    r.s_in[...] = r.wide_in[...].astype(BF)

    share(r.w_qkv, S.group_qkv, S.fw_qkv, 576)
    over_plane(r.w_attn, S.w_attn, S.group_attn)
    peers(lambda to: push(r.dm.at[b], r.dm.at[b], S.dm + b, to, s))
    sent(S.dm + b, r.dm.at[0:3])
    got(S.fw_qkv, r.w_qkv.at[:, 0:HALF])

    def turned(tile, sign, k):
        other = jnp.where(first_half, pltpu.roll(tile, 96, 1), pltpu.roll(tile, 32, 1))
        return tile * r.turn[0, k] + sign * (other * r.turn[1, k])

    def project(j):
        k = lax.rem(z + j, LINE)

        @pl.when(j > 0)
        def _():
            got(S.h1 + k, r.h1.at[0])

        x = dot(r.h1[k], r.w_qkv[:, 0:PACK])
        tiles = [x[:, 128 * t : 128 * t + 128] for t in range(5)]
        tiles[0] = turned(tiles[0], 1.0, k) * 0.125
        tiles[1] = jnp.where(low, turned(tiles[1], 1.0, k) * 0.125, tiles[1])
        tiles[2] = turned(tiles[2], 1.0, k)
        tiles[3] = turned(tiles[3], 1.0, k)
        for t in range(5):
            r.xb[0, k, :, 128 * t : 128 * t + 128] = tiles[t].astype(BF)
        push(r.xb.at[0, k], r.xb.at[1, k], S.xf + k, b, mate)

    loop(4, project)
    for k in range(4):
        sent(S.xf + k, r.xb.at[0, 0])

    spread(r.s_in, r.w_in, S.w_in)
    for k in range(4):
        got(S.xf + k, r.xb.at[0, 0])

    def tile_of(t):
        return r.xb[:, :, :, 128 * t : 128 * t + 128].reshape(1024, 128)

    heads = ((0, 2, 4, True, True), (0, 2, 4, False, False), (1, 3, 1, True, False))

    def queries(head, first, size):
        q_tile, _, _, q_low, _ = heads[head]
        q = r.xb[0, first : first + size, :, 128 * q_tile : 128 * q_tile + 128]
        return jnp.where(low if q_low else ~low, q.reshape(size * 128, 128), jnp.zeros((), BF))

    for head in range(3):
        keys, values = tile_of(heads[head][1]), tile_of(heads[head][2])
        for half in range(2):
            at = slice(256 * half, 256 * half + 256)
            scores = dot_nt(keys, queries(head, 2 * half, 2))
            weights = jnp.exp(scores - jnp.max(scores, axis=0, keepdims=True))
            weights = weights * (1.0 / jnp.sum(weights, axis=0, keepdims=True))
            weights = weights.astype(BF)
            r.pt[head, :, at] = weights
            out = dot_tn(values, weights)
            if head == 0:
                r.ot[0, 0:64, at] = out[0:64]
            elif head == 1:
                r.ot[0, 64:128, at] = out[64:128]
            else:
                r.ot[1, 0:64, at] = out[64:128]
                r.ot[1, 64:128, at] = jnp.zeros((64, 256), F32)
    for t in range(2):
        r.os[:, :, 128 * t : 128 * t + 128] = (
            r.ot[t].T.astype(BF).reshape(4, 128, 128)
        )

    stack(lambda to: push(r.os.at[to], r.ob.at[z], S.o, b, 2 * to + c))
    keep(r.os.at[z], r.ob.at[z], S.o)
    sent(S.o, r.os.at[0:3])
    share(r.w_attn, S.group_attn, S.fw_attn, 576)
    got(S.fw_attn, r.w_attn.at[:, 0:HALF])
    got(S.o, r.ob)
    a = jnp.zeros((ROWS, WIDTH), F32)
    for p in range(4):
        a += dot(r.ob[p, :, 0:128], r.w_attn[192 * p : 192 * p + 128, :])
        a += dot(r.ob[p, :, 128:192], r.w_attn[192 * p + 128 : 192 * p + 192, :])
    r.a[...] = a
    x1 = r.x0[...] + mod(2) * a
    r.x1[...] = x1
    n2, inv2 = normalize(x1)
    r.n2[...] = n2
    r.inv2[...] = jnp.broadcast_to(inv2, (ROWS, 128))
    r.h2[b] = (n2 * vec(1) * (1.0 + mod(4)) + mod(3)).astype(BF)
    peers(lambda to: push(r.h2.at[b], r.h2.at[b], S.h2 + b, to, s))
    sent(S.h2 + b, r.h2.at[0:3])
    got(S.w_out, r.w_out.at[:, 0])
    push(r.w_out.at[:, c], r.w_out.at[:, c], S.fw_out, b, mate)
    sent(S.fw_out, r.w_out.at[:, 0])
    share(r.w_in, S.w_in, S.fw_in, 768)
    got(S.fw_out, r.w_out.at[:, 0])
    got(S.fw_in, r.w_in.at[:, 0:HALF])

    def feed(j):
        k = lax.rem(b + j, DP)

        @pl.when(j > 0)
        def _():
            got(S.h2 + k, r.h2.at[0])
            got(S.dm + k, r.dm.at[0])

        u = dot(r.h2[k], r.w_in[...])
        slope = 0.7978845608028654
        cube = 0.044715
        t = jnp.tanh(slope * (u + cube * u * u * u))
        r.gb[k] = (0.5 * u * (1.0 + t)).astype(BF)
        bend = 0.5 * (1.0 + t) + 0.5 * u * (1.0 - t * t) * (slope * (1.0 + 3.0 * cube * u * u))
        r.du[k] = (dot_nt(r.dm[k], r.w_out[...].reshape(768, 768)) * bend).astype(BF)
        r.dhs[k] = dot_nt(r.du[k], r.w_in[...]).astype(BF)

        @pl.when(j > 0)
        def _():
            push(r.dhs.at[k], r.dhr.at[b], S.dh2, k, s)

    loop(4, feed)
    sent(S.dh2, r.dhs.at[0:3])

    def feed_out(j):
        k = lax.rem(b + j, DP)
        r.mms[k] = dot(r.gb[k], r.w_out[...].reshape(768, 768)).astype(BF)

        @pl.when(j > 0)
        def _():
            push(r.mms.at[k], r.mmr.at[b], S.mm, k, s)

    loop(4, feed_out)
    sent(S.mm, r.mms.at[0:3])

    def gather(own, others):
        total = own[b].astype(F32)
        for k in (1, 2, 3):
            total += others[lax.rem(b + k, DP)].astype(F32)
        return total

    for k in range(4):
        rows = slice(192 * k, 192 * k + 192)
        block = dot_tn(r.gb[:, :, rows].reshape(512, 192), r.dm[...].reshape(512, 768))
        r.g_out[k] = block.astype(BF).reshape(2, 96, 768)
    push(r.g_out.at[:, 1 - c], r.p_out, S.pair_out, b, mate)
    sent(S.pair_out, r.p_out)

    def outer(left, right, dst):
        def one(k):
            rows = pl.ds(pl.multiple_of(128 * k, 128), 128)
            result = dot_tn(
                left[:, :, rows].reshape(512, 128), right[...].reshape(512, 768)
            ).astype(BF)
            dst[0, rows, :] = result[:, 0:HALF]
            dst[1, rows, :] = result[:, HALF:WIDTH]

        loop(6, one)

    def to_mate(grad, dst, at):
        push(grad.at[1 - c], dst, at, b, mate)
        sent(at, dst)

    def pair_sum(grad, pair, at):
        got(at, pair)
        grad[c] = (grad[c].astype(F32) + pair[...].astype(F32)).astype(BF)

    def plane_sum(grad, dst, at):
        def rows(to):
            return grad.at[c, pl.ds(pl.multiple_of(192 * to, 16), 192)]

        peers(lambda to: push(rows(to), dst.at[b], at, to, s))
        keep(rows(b), dst.at[b], at)
        sent(at, dst.at[0:3])

    def line_sum(src, total, dst, first, at):
        got(first, src)
        total[...] = (
            (src[0].astype(F32) + src[1].astype(F32)) + (src[2].astype(F32) + src[3].astype(F32))
        ).astype(BF)

        def rows(to):
            return total.at[pl.ds(pl.multiple_of(48 * to, 16), 48)]

        stack(lambda to: push(rows(to), dst.at[z], at, b, 2 * to + c))
        keep(rows(z), dst.at[z], at)
        sent(at, dst.at[0:3])

    def trade(total, final, at):
        push(total.at[:, mate24], final.at[:, c], at, b, mate)
        sent(at, final.at[:, 0])
        final[:, c] = total[:, own24, :]

    outer(r.h2, r.du, r.g_in)
    to_mate(r.g_in, r.p_in, S.pair_in)

    got(S.pair_out, r.p_out)
    for k in range(4):
        r.g_out[k, c] = (r.g_out[k, c].astype(F32) + r.p_out[k].astype(F32)).astype(BF)

    def send_gout(to):
        push(r.g_out.at[to, c], r.r_out.at[z], S.line_out, b, 2 * to + c)

    stack(send_gout)
    keep(r.g_out.at[z, c], r.r_out.at[z], S.line_out)
    sent(S.line_out, r.r_out.at[0:3])

    got(S.dh2, r.dhr.at[0:3])
    dh = gather(r.dhs, r.dhr)
    n2 = r.n2[...]
    inv2 = r.inv2[:, 0:1]
    r.early[...] = jnp.zeros((8, 768), F32)
    r.early[2:3, :] = jnp.sum(dh, axis=0, keepdims=True)
    both = jnp.sum(dh * n2, axis=0, keepdims=True)
    r.early[3:4, :] = both * vec(1)
    r.early[0:1, :] = both * (1.0 + mod(4))
    grad = dh * ((1.0 + mod(4)) * vec(1))
    dx1 = i_cot[0].astype(F32) + norm_back(n2, inv2, grad)
    r.dx1[...] = dx1
    r.early[1:2, :] = jnp.sum(dx1 * r.a[...], axis=0, keepdims=True)
    r.das[...] = (dx1 * mod(2)).astype(BF)
    for p in range(4):
        first = 192 * p
        r.dos[p, :, 0:128] = dot_nt(r.das[...], r.w_attn[first : first + 128, :]).astype(BF)
        tail = dot_nt(r.das[...], r.w_attn[first + 128 : first + 192, :])
        r.dos[p, :, 128:256] = jnp.concatenate(
            [tail, jnp.zeros((ROWS, 64), F32)], axis=1
        ).astype(BF)

    stack(lambda to: push(r.dos.at[to], r.dob.at[z], S.do, b, 2 * to + c))
    keep(r.dos.at[z], r.dob.at[z], S.do)
    sent(S.do, r.dos.at[0:3])

    for p in range(4):
        rows = slice(192 * p, 192 * p + 192)
        result = dot_tn(r.ob[p], r.das[...])[0:192].astype(BF)
        r.g_attn[0, rows, :] = result[:, 0:HALF]
        r.g_attn[1, rows, :] = result[:, HALF:WIDTH]
    to_mate(r.g_attn, r.p_attn, S.pair_attn)

    got(S.mm, r.mmr.at[0:3])
    mm = gather(r.mms, r.mmr)
    o_y[...] = (r.x1[...] + mod(5) * mm).astype(BF)
    r.early[4:5, :] = jnp.sum(i_cot[0].astype(F32) * mm, axis=0, keepdims=True)

    def over_line(src, dst, name):
        def one(k):
            push(src, dst.at[s], name, b, lax.rem(s + k, SEQ))

        loop(SEQ, one, 1)
        keep(src, dst.at[s], name)
        sent(name, dst.at[0:7])

    def over_group(got_ref, dst, name):
        total = got_ref[0]
        for k in range(1, SEQ):
            total += got_ref[k]
        dst[b] = total
        peers(lambda to: push(dst.at[b], dst.at[b], name, to, s))
        sent(name, dst.at[0:3])

    over_line(r.early, r.early_got, S.early)

    pair_sum(r.g_in, r.p_in, S.pair_in)

    def send_gin(k):
        to = lax.rem(chip + k, CHIPS)
        push(
            r.g_in.at[c, pl.ds(pl.multiple_of(48 * to, 16), 48)],
            r.r_in.at[chip],
            S.line_in,
            lax.div(to, LINE),
            2 * lax.rem(to, LINE) + c,
        )

    loop(CHIPS, send_gin, 1)
    keep(r.g_in.at[c, chip_rows], r.r_in.at[chip], S.line_in)
    sent(S.line_in, r.r_in.at[0:15])
    pair_sum(r.g_attn, r.p_attn, S.pair_attn)
    plane_sum(r.g_attn, r.q_attn, S.plane_attn)

    got(S.do, r.dob)
    dot0, dot1 = r.dob[:, :, 0:128].reshape(512, 128), r.dob[:, :, 128:256].reshape(512, 128)
    zero = jnp.zeros((), BF)
    moved = pltpu.roll(dot1.astype(F32), 64, 1).astype(BF)
    grads = (jnp.where(low, dot0, zero), jnp.where(low, zero, dot0), moved)
    product = dot0.astype(F32).T * r.ot[0]
    deltas = (
        jnp.sum(product[0:64], axis=0, keepdims=True),
        jnp.sum(product[64:128], axis=0, keepdims=True),
        jnp.sum(dot1.astype(F32).T * r.ot[1], axis=0, keepdims=True),
    )
    turned_q = []
    for head in range(3):
        keys, values = tile_of(heads[head][1]), tile_of(heads[head][2])
        for half in range(2):
            at = slice(256 * half, 256 * half + 256)
            dp = dot_nt(values, grads[head][at])
            ds = (r.pt[head, :, at].astype(F32) * (dp - deltas[head][:, at])).astype(BF)
            r.dst[:, at] = ds
            turned_q.append(dot_tn(keys, ds))
        dk = dot(r.dst[...], queries(head, 0, 4))
        dv = dot(r.pt[head], grads[head])
        if head == 0:
            r.ga[:, 256:384] = dk
            r.ga[:, 512:640] = dv
        elif head == 1:
            r.ga[:, 256:384] += dk
            r.ga[:, 512:640] += dv
        else:
            r.ga[:, 384:512] = dk
            r.ga[:, 128:256] = dv
    r.gps[...] = r.ga[512:1024, 128:640].astype(BF)
    push(r.gps, r.gpr, S.gp, b, mate)
    sent(S.gp, r.gps)
    for half in range(2):
        at = slice(256 * half, 256 * half + 256)
        top = jnp.concatenate([turned_q[half][0:64], turned_q[2 + half][64:128]], axis=0)
        r.ga[at, 0:128] = top.T * 0.125
        r.ga[at, 128:256] += turned_q[4 + half].T * 0.125
    got(S.gp, r.gpr)

    def unproject(j):
        k = lax.rem(z + 1 + j, LINE)
        rows = pl.ds(pl.multiple_of(128 * k, 128), 128)
        tiles = [r.ga[rows, 0:128]] + [
            r.ga[rows, 128 * t : 128 * t + 128]
            + r.gpr[rows, 128 * t - 128 : 128 * t].astype(F32)
            for t in range(1, 5)
        ]
        tiles[0] = turned(tiles[0], -1.0, k)
        tiles[1] = jnp.where(low, turned(tiles[1], -1.0, k), tiles[1])
        tiles[2] = turned(tiles[2], -1.0, k)
        tiles[3] = turned(tiles[3], -1.0, k)
        for t in range(5):
            r.dqkv[k, :, 128 * t : 128 * t + 128] = tiles[t].astype(BF)
        r.dqkv[k, :, PACK:WIDTH] = jnp.zeros((128, 128), BF)
        r.d1s[k] = dot_nt(r.dqkv[k, :, 0:PACK], r.w_qkv[:, 0:PACK]).astype(BF)

        @pl.when(j < 3)
        def _():
            push(r.d1s.at[k], r.d1r.at[z], S.dh1, b, 2 * k + c)

    loop(4, unproject)
    sent(S.dh1, r.d1s.at[0:3])
    outer(r.h1, r.dqkv, r.g_qkv)
    to_mate(r.g_qkv, r.p_qkv, S.pair_qkv)
    line_sum(r.q_attn, r.m_attn, r.r_attn, S.plane_attn, S.line_attn)
    got(S.early, r.early_got)
    over_group(r.early_got, r.early_all, S.early2)
    pair_sum(r.g_qkv, r.p_qkv, S.pair_qkv)
    plane_sum(r.g_qkv, r.q_qkv, S.plane_qkv)

    got(S.line_in, r.r_in)
    for p in range(4):
        r.t_in[p] = (r.r_in[4 * p].astype(F32) + r.r_in[4 * p + 1].astype(F32)) + (
            r.r_in[4 * p + 2].astype(F32) + r.r_in[4 * p + 3].astype(F32)
        )
    trade(r.t_in, r.f_in, S.last_in)
    line_sum(r.q_qkv, r.m_qkv, r.r_qkv, S.plane_qkv, S.line_qkv)

    got(S.dh1, r.d1r.at[0:3])
    dh = r.d1s[z].astype(F32)
    for k in (1, 2, 3):
        dh += r.d1r[lax.rem(z + k, LINE)].astype(F32)
    n1 = r.n1[...]
    both = jnp.sum(dh * n1, axis=0, keepdims=True)
    r.late[0:1, :] = both * (1.0 + mod(1))
    r.late[1:2, :] = jnp.sum(dh, axis=0, keepdims=True)
    r.late[2:3, :] = both * vec(0)
    grad = dh * ((1.0 + mod(1)) * vec(0))
    dx0 = r.dx1[...] + norm_back(n1, r.inv1[:, 0:1], grad)
    o_dx[...] = jnp.where(hidden, 0.0, dx0)
    r.late[3:4, :] = jnp.sum(jnp.where(hidden, dx0, 0.0), axis=0, keepdims=True)
    over_line(r.late, r.late_got, S.late)

    got(S.line_out, r.r_out)
    total = (r.r_out[0].astype(F32) + r.r_out[1].astype(F32)) + (
        r.r_out[2].astype(F32) + r.r_out[3].astype(F32)
    )
    o_gout[...] = total
    squares = total * total
    squares = jnp.sum(squares[:, 0:128] + squares[:, 128:256] + squares[:, 256:384]
                      + squares[:, 384:512] + squares[:, 512:640] + squares[:, 640:768],
                      axis=0, keepdims=True)

    def fold(value):
        total = value[:, 0:128] * value[:, 0:128]
        for t in range(1, value.shape[1] // 128):
            total += value[:, 128 * t : 128 * t + 128] * value[:, 128 * t : 128 * t + 128]
        return jnp.sum(total, axis=0, keepdims=True)

    got(S.line_attn, r.r_attn)
    r.t_attn[0] = (r.r_attn[0].astype(F32) + r.r_attn[1].astype(F32)) + (
        r.r_attn[2].astype(F32) + r.r_attn[3].astype(F32)
    )
    trade(r.t_attn, r.f_attn, S.last_attn)
    got(S.line_qkv, r.r_qkv)
    r.t_qkv[...] = r.r_qkv[...].astype(F32)
    trade(r.t_qkv, r.f_qkv, S.last_qkv)
    got(S.late, r.late_got)
    over_group(r.late_got, r.late_all, S.late2)
    got(S.last_in, r.f_in.at[:, 0])
    got(S.last_attn, r.f_attn.at[:, 0])
    for h in range(2):
        for p in range(4):
            value = r.f_in[p, h]
            o_gin[:, 768 * p + 384 * h : 768 * p + 384 * h + 384] = value
            squares += fold(value)
        value = r.f_attn[0, h]
        o_gattn[:, 384 * h : 384 * h + 384] = value
        squares += fold(value)
    got(S.last_qkv, r.f_qkv.at[:, 0])
    where = {which: index for index, which in enumerate(HALVES) if which is not None}

    def packed_half(chunk, high):
        kind, rest = chunk // 12, chunk % 12
        index = where[(kind, rest % 3)]
        t = index // 2
        tile = r.f_qkv[rest // 3, t // 3, :, t % 3 * 128 : t % 3 * 128 + 128]
        return tile if index % 2 == high else pltpu.roll(tile, 64, 1)

    for t in range(18):
        o_gqkv[:, 128 * t : 128 * t + 128] = jnp.where(
            low, packed_half(2 * t, 0), packed_half(2 * t + 1, 1)
        )
    for p in range(4):
        for h in range(2):
            squares += fold(r.f_qkv[p, h])

    r.sq[me] = squares

    def send_sq(k):
        other = lax.rem(me + k, ALL)
        push(r.sq.at[me], r.sq.at[me], S.sq, lax.div(other, SEQ), lax.rem(other, SEQ))

    loop(ALL, send_sq, 1)
    sent(S.sq, r.sq.at[0:31])
    got(S.early2, r.early_all.at[0:3])
    got(S.late2, r.late_all.at[0:3])
    mods = []
    for k in range(4):
        early, late = r.early_all[k], r.late_all[k]
        rows = jnp.concatenate([late[1:3], early[1:5], jnp.zeros((2, 768), F32)], axis=0)
        for n in range(6):
            for m in range(6):
                r.dmod_flat[k, 6 * n + m : 6 * n + m + 1, :] = rows[
                    n : n + 1, 128 * m : 128 * m + 128
                ]
        mods.append(rows)
    gain = jnp.concatenate(
        [
            sum(r.late_all[k][0:1] for k in range(4)),
            sum(r.early_all[k][0:1] for k in range(4)),
            (mods[0] + mods[1] + mods[2] + mods[3])[0:6],
        ],
        axis=0,
    )
    mask_row = sum(r.late_all[k][3:4] for k in range(4))
    gains = jnp.concatenate([gain, mask_row, jnp.zeros((7, 768), F32)], axis=0)
    masters = jnp.concatenate([i_vec[...], jnp.zeros((7, 768), F32)], axis=0)
    own = lax.rem(WIDTH - 24 * me, WIDTH)
    o_gvec[...] = pltpu.roll(gains, own, 1)[:, 0:128]
    o_vec[...] = pltpu.roll(masters, own, 1)[:, 0:128]
    r.mod_pad[...] = jnp.zeros((8, 384), F32)
    window = lax.div(wide * me, 128)
    for k in range(4):
        rows = r.dmod_flat[k, pl.ds(window, 3), :]
        for m in range(3):
            r.mod_pad[k : k + 1, 128 * m : 128 * m + 128] = rows[m : m + 1, :]
    o_dmod[...] = pltpu.roll(r.mod_pad[...], lax.rem(384 - lax.rem(wide * me, 128), 384), 1)[:, 0:256]
    small = jnp.sum(gain * gain) + jnp.sum(mask_row * mask_row)
    conds = [r.conds_all[k][0:1].astype(BF).astype(F32) for k in range(4)]
    for k in range(4):
        for m in range(k, 4):
            term = jnp.sum(mods[k] * mods[m]) * jnp.sum(conds[k] * conds[m])
            small += term if m == k else 2.0 * term
    got(S.sq, r.sq.at[0:31])
    total = r.sq[0]
    for k in range(1, ALL):
        total += r.sq[k]
    o_norm[...] = jnp.broadcast_to(jnp.sqrt(jnp.sum(total) + small), (8, 128))

    for at, like in drains:
        left(at, like)


def run_layer(*args):
    shapes = (
        ((ROWS, WIDTH), BF),
        ((ROWS, WIDTH), F32),
        ((8, 128), F32),
        ((24, 3 * WIDTH), F32),
        ((24, WIDTH), F32),
        ((24, 4 * WIDTH), F32),
        ((96, WIDTH), F32),
        ((8, 256), F32),
        ((16, 128), F32),
        ((16, 128), F32),
        ((8, 128), F32),
    )
    whole = pl.BlockSpec(memory_space=pltpu.VMEM)
    scalar = pl.BlockSpec(memory_space=pltpu.SMEM)
    return pl.pallas_call(
        layer_kernel,
        out_shape=[jax.ShapeDtypeStruct(shape, kind) for shape, kind in shapes],
        in_specs=[scalar] * 3 + [whole] * (len(args) - 3),
        out_specs=[whole] * len(shapes),
        scratch_shapes=[pltpu.VMEM(shape, kind) for shape, kind in SCRATCH.values()]
        + [pltpu.SemaphoreType.DMA((SEM_COUNT,)), pltpu.SemaphoreType.DMA((SEM_COUNT,))],
        compiler_params=pltpu.CompilerParams(
            collective_id=0, has_side_effects=True, vmem_limit_bytes=60 * 1024 * 1024
        ),
    )(*args)


def finish_kernel(
    y, dx, norm, g_qkv, g_attn, g_in, g_out, dmod, g_vec, own_vec, conds, *rest
):
    (w_ada, w_qkv, w_attn, w_in, w_out), moments, outs = rest[:5], rest[5:17], rest[17:]
    outs[0][0] = y[...]
    outs[1][0] = dx[...]
    outs[2][0, 0] = norm[0, 0]
    clip = jnp.minimum(1.0, CLIP / (norm[0:1, 0:1] + 1e-06))
    columns = w_ada.shape[1]
    turned_conds = conds[...].astype(BF).astype(F32).T
    g_ada = turned_conds[:, 0:1] * dmod[0:1, 0:columns]
    for k in range(1, 4):
        g_ada += turned_conds[:, k : k + 1] * dmod[k : k + 1, 0:columns]
    narrow = moments[0].shape[1]
    grads = (
        g_vec[0:9, 0:narrow],
        g_ada,
        g_qkv[...],
        g_attn[...],
        g_in[...],
        g_out[...],
    )
    weights = (
        own_vec[0:9, 0:narrow],
        w_ada[...],
        w_qkv[...],
        w_attn[...],
        w_in[...],
        w_out[...],
    )
    for k in range(6):
        results = adam_step(
            weights[k],
            grads[k] * clip,
            moments[2 * k][...],
            moments[2 * k + 1][...],
            RATE if k else RATE_VECTORS,
            DECAY if k else 0.0,
        )
        for n in range(3):
            outs[3 + 3 * k + n][...] = results[n]


def run_finish(partial_results, weights, moments):
    shapes = [((1, ROWS, WIDTH), BF), ((1, ROWS, WIDTH), F32), ((1, 1), F32)]
    for moment in moments[::2]:
        shapes += [(moment.shape, F32)] * 3
    whole = pl.BlockSpec(memory_space=pltpu.VMEM)
    specs = [whole] * len(shapes)
    specs[2] = pl.BlockSpec(memory_space=pltpu.SMEM)
    args = (*partial_results, *weights, *moments)
    return pl.pallas_call(
        finish_kernel,
        out_shape=[jax.ShapeDtypeStruct(shape, kind) for shape, kind in shapes],
        in_specs=[whole] * len(args),
        out_specs=specs,
        compiler_params=pltpu.CompilerParams(vmem_limit_bytes=32 * 1024 * 1024),
    )(*args)


def slices(
    tokens_in,
    cotangent,
    timesteps,
    span_start,
    span_len,
    vectors,
    w_ada,
    w_qkv,
    w_attn,
    w_in,
    w_out,
    m_vec,
    v_vec,
    m_ada,
    v_ada,
    m_qkv,
    v_qkv,
    m_attn,
    v_attn,
    m_in,
    v_in,
    m_out,
    v_out,
):
    partial_results = run_layer(
        timesteps,
        span_start,
        span_len,
        tokens_in,
        cotangent,
        vectors,
        w_ada,
        w_qkv,
        w_attn,
        w_in,
        w_out,
    )
    moments = (
        m_vec,
        v_vec,
        m_ada,
        v_ada,
        m_qkv,
        v_qkv,
        m_attn,
        v_attn,
        m_in,
        v_in,
        m_out,
        v_out,
    )
    results = run_finish(partial_results, (w_ada, w_qkv, w_attn, w_in, w_out), moments)
    return (results[0], results[1], results[2].reshape(()), *results[3:])


def solution(mesh):
    in_specs = (
        P("dp", "seq", None),
        P("dp", "seq", None),
        P("dp"),
        P("dp"),
        P("dp"),
        P(),
        P(None, ("dp", "seq")),
        P(("dp", "seq"), None),
        P(("dp", "seq"), None),
        P(("dp", "seq"), None),
        P(("dp", "seq"), None),
        P(None, ("dp", "seq")),
        P(None, ("dp", "seq")),
        P(None, ("dp", "seq")),
        P(None, ("dp", "seq")),
        P(("dp", "seq"), None),
        P(("dp", "seq"), None),
        P(("dp", "seq"), None),
        P(("dp", "seq"), None),
        P(("dp", "seq"), None),
        P(("dp", "seq"), None),
        P(("dp", "seq"), None),
        P(("dp", "seq"), None),
    )
    out_specs = (
        P("dp", "seq", None),
        P("dp", "seq", None),
        P(),
        P(None, ("dp", "seq")),
        P(None, ("dp", "seq")),
        P(None, ("dp", "seq")),
        P(None, ("dp", "seq")),
        P(None, ("dp", "seq")),
        P(None, ("dp", "seq")),
        P(("dp", "seq"), None),
        P(("dp", "seq"), None),
        P(("dp", "seq"), None),
        P(("dp", "seq"), None),
        P(("dp", "seq"), None),
        P(("dp", "seq"), None),
        P(("dp", "seq"), None),
        P(("dp", "seq"), None),
        P(("dp", "seq"), None),
        P(("dp", "seq"), None),
        P(("dp", "seq"), None),
        P(("dp", "seq"), None),
    )
    sizes = dict(mesh.shape)
    local = slices if (sizes["dp"], sizes["seq"]) == (4, 8) else plain
    return jax.shard_map(local, mesh=mesh, in_specs=in_specs, out_specs=out_specs, check_vma=False)
```

```python
from functools import partial
import math
from types import SimpleNamespace

import jax
import jax.numpy as jnp
from jax import lax
from jax.experimental import pallas as pl
from jax.experimental.pallas import tpu as pltpu
from jax.sharding import PartitionSpec as P

HD = 64
COND = 128
STEP = 10


BETA_ONE = 0.9
BETA_TWO = 0.999
ADAM_EPS = 1e-08
RATE = 0.1
RATE_VECTORS = 0.3
DECAY = 0.01
CLIP = 1.0
NORM_EPS = 1e-05


def cond_input(timesteps):
    half_cond = COND // 2
    freqs = jnp.exp(jnp.arange(half_cond, dtype=jnp.float32) * (-math.log(10000.0) / half_cond))
    angles = timesteps.astype(jnp.float32)[:, None] * freqs[None, :]
    return jax.nn.silu(jnp.concatenate([jnp.cos(angles), jnp.sin(angles)], axis=1))


def rotary_tables(positions):
    half_head = HD // 2
    inverse = jnp.exp(jnp.arange(half_head, dtype=jnp.float32) * (-math.log(10000.0) / half_head))
    angles = positions.astype(jnp.float32)[:, None] * inverse[None, :]
    return (jnp.cos(angles), jnp.sin(angles))


def rotate(values, cosines, sines):
    half_head = values.shape[-1] // 2
    first = values[..., :half_head]
    second = values[..., half_head:]
    cos_b = cosines[:, None, :]
    sin_b = sines[:, None, :]
    return jnp.concatenate(
        [first * cos_b - second * sin_b, second * cos_b + first * sin_b], axis=-1
    )


def rotate_back(grads, cosines, sines):
    half_head = grads.shape[-1] // 2
    first = grads[..., :half_head]
    second = grads[..., half_head:]
    cos_b = cosines[:, None, :]
    sin_b = sines[:, None, :]
    return jnp.concatenate(
        [first * cos_b + second * sin_b, second * cos_b - first * sin_b], axis=-1
    )


def normalize(values):
    centre = jnp.mean(values, axis=-1, keepdims=True)
    centred = values - centre
    inverse = lax.rsqrt(jnp.mean(centred * centred, axis=-1, keepdims=True) + NORM_EPS)
    return (centred * inverse, inverse)


def norm_back(normed, inverse, grad):
    return inverse * (
        grad
        - jnp.mean(grad, axis=-1, keepdims=True)
        - normed * jnp.mean(grad * normed, axis=-1, keepdims=True)
    )


def split_kv(block, width):
    seqs, block_rows = (block.shape[0], block.shape[1])
    keys = block[..., :width].reshape(seqs, block_rows, width // HD, HD)
    values = block[..., width:].reshape(seqs, block_rows, width // HD, HD)
    return (keys, values)


def attend_piece(carry, piece, queries, width, factor):
    piece_rows = piece.shape[1]
    size = math.gcd(piece_rows, 512)

    def attend_one_block(index, state):
        running, denom, accum = state
        block = lax.dynamic_slice_in_dim(piece, index * size, size, 1)
        keys, values = split_kv(block, width)
        scores = (
            jnp.einsum("sqhd,skhd->shqk", queries, keys, preferred_element_type=jnp.float32)
            * factor
        )
        highest = jnp.maximum(running, jnp.max(scores, axis=-1))
        shrink = jnp.exp(running - highest)
        weights = jnp.exp(scores - highest[..., None])
        denom = denom * shrink + jnp.sum(weights, axis=-1)
        accum = accum * shrink[..., None] + jnp.einsum(
            "shqk,skhd->shqd",
            weights.astype(jnp.bfloat16),
            values,
            preferred_element_type=jnp.float32,
        )
        return (highest, denom, accum)

    return lax.fori_loop(0, piece_rows // size, attend_one_block, carry)


def block_grads(block, queries, grad_out, logsum, delta, width, factor):
    keys, values = split_kv(block, width)
    scores = (
        jnp.einsum("sqhd,skhd->shqk", queries, keys, preferred_element_type=jnp.float32) * factor
    )
    probs = jnp.exp(scores - logsum[..., None])
    dprobs = jnp.einsum("sqhd,skhd->shqk", grad_out, values, preferred_element_type=jnp.float32)
    dscores = (probs * (dprobs - delta[..., None])).astype(jnp.bfloat16)
    return (keys, probs, dscores)


def query_grads(kv_all, queries, grad_out, logsum, delta, width, factor):
    total_rows = kv_all.shape[1]
    size = math.gcd(total_rows, 512)

    def query_one_block(index, accum):
        block = lax.dynamic_slice_in_dim(kv_all, index * size, size, 1)
        keys, probs, dscores = block_grads(block, queries, grad_out, logsum, delta, width, factor)
        return accum + factor * jnp.einsum(
            "shqk,skhd->sqhd", dscores, keys, preferred_element_type=jnp.float32
        )

    return lax.fori_loop(
        0, total_rows // size, query_one_block, jnp.zeros(queries.shape, jnp.float32)
    )


def key_grads(kv_all, queries, grad_out, logsum, delta, width, factor, count):
    size = math.gcd(count, 512)
    seqs = queries.shape[0]

    def key_one_block(index, accum):
        block = lax.dynamic_slice_in_dim(kv_all, index * size, size, 1)
        keys, probs, dscores = block_grads(block, queries, grad_out, logsum, delta, width, factor)
        grad_vals = jnp.einsum(
            "shqk,sqhd->skhd",
            probs.astype(jnp.bfloat16),
            grad_out,
            preferred_element_type=jnp.float32,
        )
        grad_keys = factor * jnp.einsum(
            "shqk,sqhd->skhd", dscores, queries, preferred_element_type=jnp.float32
        )
        joined = jnp.concatenate(
            [grad_keys.reshape(seqs, size, width), grad_vals.reshape(seqs, size, width)], axis=-1
        )
        return lax.dynamic_update_slice_in_dim(
            accum, jnp.transpose(joined, (1, 0, 2)), index * size, 0
        )

    initial = jnp.zeros((count, seqs, 2 * width), jnp.float32)
    return lax.fori_loop(0, count // size, key_one_block, initial)


def adam_step(weight, grad, first, second, rate, decay_rate):
    new_first = BETA_ONE * first + (1.0 - BETA_ONE) * grad
    new_second = BETA_TWO * second + (1.0 - BETA_TWO) * grad * grad
    fixed_first = new_first / (1.0 - BETA_ONE**STEP)
    fixed_second = new_second / (1.0 - BETA_TWO**STEP)
    new_weight = weight - rate * (
        fixed_first / (jnp.sqrt(fixed_second) + ADAM_EPS) + decay_rate * weight
    )
    return (new_first, new_second, new_weight)


def mod_back(grad_hidden, ln_values, normed, scale_part, gain):
    grad_shift = jnp.sum(grad_hidden, axis=1)
    grad_scale = jnp.sum(grad_hidden * ln_values, axis=1)
    grad_ln = grad_hidden * (1.0 + scale_part)
    grad_gain = jnp.sum(grad_ln * normed, axis=(0, 1))
    return (grad_shift, grad_scale, grad_gain, grad_ln * gain)


def plain(
    tokens_in,
    cotangent,
    timesteps,
    span_start,
    span_len,
    vectors,
    w_ada,
    w_qkv,
    w_attn,
    w_in,
    w_out,
    m_vec,
    v_vec,
    m_ada,
    v_ada,
    m_qkv,
    v_qkv,
    m_attn,
    v_attn,
    m_in,
    v_in,
    m_out,
    v_out,
):
    seqs, group, width = tokens_in.shape
    heads = width // HD
    factor = HD ** (-0.5)
    flat_rows = seqs * group
    full_ada, full_qkv, full_attn, full_in, full_out = (
        lax.all_gather(w_ada.astype(jnp.bfloat16), ("dp", "seq"), axis=1, tiled=True),
        lax.all_gather(w_qkv.astype(jnp.bfloat16), ("dp", "seq"), axis=0, tiled=True),
        lax.all_gather(w_attn.astype(jnp.bfloat16), ("dp", "seq"), axis=0, tiled=True),
        lax.all_gather(w_in.astype(jnp.bfloat16), ("dp", "seq"), axis=0, tiled=True),
        lax.all_gather(w_out.astype(jnp.bfloat16), ("dp", "seq"), axis=0, tiled=True),
    )
    positions = lax.axis_index("seq") * group + jnp.arange(group, dtype=jnp.int32)
    masked = (positions[None, :] >= span_start[:, None]) & (
        positions[None, :] < (span_start + span_len)[:, None]
    )
    cond_bf = cond_input(timesteps).astype(jnp.bfloat16)
    modulation = jnp.dot(cond_bf, full_ada, preferred_element_type=jnp.float32) + vectors[
        2:8
    ].reshape(1, 6 * width)
    pieces = [modulation[:, which * width : (which + 1) * width][:, None, :] for which in range(6)]
    shift_one, scale_one, gate_one, shift_two, scale_two, gate_two = pieces
    start_tokens = jnp.where(
        masked[..., None], vectors[8][None, None, :], tokens_in.astype(jnp.float32)
    )
    normed_one, inv_one = normalize(start_tokens)
    ln_one = normed_one * vectors[0]
    hidden_one = (
        (ln_one * (1.0 + scale_one) + shift_one).astype(jnp.bfloat16).reshape(flat_rows, width)
    )
    projected = jnp.dot(hidden_one, full_qkv, preferred_element_type=jnp.float32).reshape(
        seqs, group, 3 * width
    )
    cosines, sines = rotary_tables(positions)
    queries = rotate(projected[..., :width].reshape(seqs, group, heads, HD), cosines, sines).astype(
        jnp.bfloat16
    )
    keys_here = rotate(
        projected[..., width : 2 * width].reshape(seqs, group, heads, HD), cosines, sines
    ).astype(jnp.bfloat16)
    values_here = projected[..., 2 * width :].astype(jnp.bfloat16)
    kv_local = jnp.concatenate([keys_here.reshape(seqs, group, width), values_here], axis=-1)
    initial = (
        jnp.full((seqs, heads, group), -1e30, jnp.float32),
        jnp.zeros((seqs, heads, group), jnp.float32),
        jnp.zeros((seqs, heads, group, HD), jnp.float32),
    )
    running, denom, accum = attend_piece(
        initial, lax.all_gather(kv_local, "seq", axis=1, tiled=True), queries, width, factor
    )
    attn_heads = accum / denom[..., None]
    logsum = running + jnp.log(denom)
    attn_rows = jnp.transpose(attn_heads, (0, 2, 1, 3)).reshape(flat_rows, width)
    attn_bf = attn_rows.astype(jnp.bfloat16)
    branch_one = jnp.dot(attn_bf, full_attn, preferred_element_type=jnp.float32).reshape(
        seqs, group, width
    )
    mid_tokens = start_tokens + gate_one * branch_one
    normed_two, inv_two = normalize(mid_tokens)
    ln_two = normed_two * vectors[1]
    hidden_two = (
        (ln_two * (1.0 + scale_two) + shift_two).astype(jnp.bfloat16).reshape(flat_rows, width)
    )
    pre_act = jnp.dot(hidden_two, full_in, preferred_element_type=jnp.float32)
    activ, gelu_back = jax.vjp(partial(jax.nn.gelu, approximate=True), pre_act)
    activ_bf = activ.astype(jnp.bfloat16)
    branch_two = jnp.dot(activ_bf, full_out, preferred_element_type=jnp.float32).reshape(
        seqs, group, width
    )
    block_out = (mid_tokens + gate_two * branch_two).astype(jnp.bfloat16)
    grad_y = cotangent.astype(jnp.float32)
    grad_gate_two = jnp.sum(grad_y * branch_two, axis=1)
    grad_branch_two = (grad_y * gate_two).astype(jnp.bfloat16).reshape(flat_rows, width)
    grad_w_out = jnp.dot(activ_bf.T, grad_branch_two, preferred_element_type=jnp.float32)
    grad_activ = jnp.dot(grad_branch_two, full_out.T, preferred_element_type=jnp.float32)
    grad_pre = gelu_back(grad_activ)[0].astype(jnp.bfloat16)
    grad_w_in = jnp.dot(hidden_two.T, grad_pre, preferred_element_type=jnp.float32)
    grad_hidden_two = jnp.dot(grad_pre, full_in.T, preferred_element_type=jnp.float32).reshape(
        seqs, group, width
    )
    grad_shift_two, grad_scale_two, grad_gain_two, grad_normed_two = mod_back(
        grad_hidden_two, ln_two, normed_two, scale_two, vectors[1]
    )
    grad_mid = grad_y + norm_back(normed_two, inv_two, grad_normed_two)
    grad_gate_one = jnp.sum(grad_mid * branch_one, axis=1)
    grad_branch_one = (grad_mid * gate_one).astype(jnp.bfloat16).reshape(flat_rows, width)
    grad_w_attn = jnp.dot(attn_bf.T, grad_branch_one, preferred_element_type=jnp.float32)
    grad_attn_bf = (
        jnp.dot(grad_branch_one, full_attn.T, preferred_element_type=jnp.float32)
        .astype(jnp.bfloat16)
        .reshape(seqs, group, heads, HD)
    )
    delta = jnp.einsum("sqhd,shqd->shq", grad_attn_bf.astype(jnp.float32), attn_heads)
    kv_all = lax.all_gather(kv_local, "seq", axis=1, tiled=True)
    grad_queries = query_grads(kv_all, queries, grad_attn_bf, logsum, delta, width, factor)
    grad_kv = jnp.transpose(
        lax.psum_scatter(
            key_grads(
                kv_all,
                queries,
                grad_attn_bf,
                logsum,
                delta,
                width,
                factor,
                group * lax.axis_size("seq"),
            ).astype(jnp.bfloat16),
            "seq",
            scatter_dimension=0,
            tiled=True,
        ).astype(jnp.float32),
        (1, 0, 2),
    )
    grad_keys = grad_kv[..., :width].reshape(seqs, group, heads, HD)
    grad_qkv = jnp.concatenate(
        [
            rotate_back(grad_queries, cosines, sines).reshape(seqs, group, width),
            rotate_back(grad_keys, cosines, sines).reshape(seqs, group, width),
            grad_kv[..., width:],
        ],
        axis=-1,
    )
    grad_qkv = grad_qkv.astype(jnp.bfloat16).reshape(flat_rows, 3 * width)
    grad_w_qkv = jnp.dot(hidden_one.T, grad_qkv, preferred_element_type=jnp.float32)
    grad_hidden_one = jnp.dot(grad_qkv, full_qkv.T, preferred_element_type=jnp.float32).reshape(
        seqs, group, width
    )
    grad_shift_one, grad_scale_one, grad_gain_one, grad_normed_one = mod_back(
        grad_hidden_one, ln_one, normed_one, scale_one, vectors[0]
    )
    grad_start = grad_mid + norm_back(normed_one, inv_one, grad_normed_one)
    grad_mask_row = jnp.sum(jnp.where(masked[..., None], grad_start, 0.0), axis=(0, 1))
    grad_input = jnp.where(masked[..., None], 0.0, grad_start)
    grad_mod = jnp.concatenate(
        [
            grad_shift_one,
            grad_scale_one,
            grad_gate_one,
            grad_shift_two,
            grad_scale_two,
            grad_gate_two,
        ],
        axis=1,
    )
    grad_w_ada = jnp.dot(cond_bf.astype(jnp.float32).T, grad_mod, precision=lax.Precision.HIGHEST)
    grad_vectors = jnp.concatenate(
        [
            grad_gain_one[None, :],
            grad_gain_two[None, :],
            jnp.sum(grad_mod, axis=0).reshape(6, width),
            grad_mask_row[None, :],
        ],
        axis=0,
    )
    red_ada, red_qkv, red_attn, red_in, red_out, red_vec = (
        lax.psum_scatter(grad_w_ada, ("dp", "seq"), scatter_dimension=1, tiled=True),
        lax.psum_scatter(grad_w_qkv, ("dp", "seq"), scatter_dimension=0, tiled=True),
        lax.psum_scatter(grad_w_attn, ("dp", "seq"), scatter_dimension=0, tiled=True),
        lax.psum_scatter(grad_w_in, ("dp", "seq"), scatter_dimension=0, tiled=True),
        lax.psum_scatter(grad_w_out, ("dp", "seq"), scatter_dimension=0, tiled=True),
        lax.psum_scatter(grad_vectors, ("dp", "seq"), scatter_dimension=1, tiled=True),
    )
    local_squares = jnp.float32(0.0)
    for reduced in (red_vec, red_ada, red_qkv, red_attn, red_in, red_out):
        local_squares = local_squares + jnp.sum(reduced * reduced)
    grad_norm = jnp.sqrt(lax.psum(local_squares, ("dp", "seq")))
    clip_factor = jnp.minimum(1.0, CLIP / (grad_norm + 1e-06))
    columns = red_vec.shape[1]
    own_vectors = lax.dynamic_slice_in_dim(
        vectors, lax.axis_index(("dp", "seq")) * columns, columns, 1
    )
    vec_out = adam_step(own_vectors, red_vec * clip_factor, m_vec, v_vec, RATE_VECTORS, 0.0)
    ada_out = adam_step(w_ada, red_ada * clip_factor, m_ada, v_ada, RATE, DECAY)
    qkv_out = adam_step(w_qkv, red_qkv * clip_factor, m_qkv, v_qkv, RATE, DECAY)
    attn_out = adam_step(w_attn, red_attn * clip_factor, m_attn, v_attn, RATE, DECAY)
    in_out = adam_step(w_in, red_in * clip_factor, m_in, v_in, RATE, DECAY)
    out_out = adam_step(w_out, red_out * clip_factor, m_out, v_out, RATE, DECAY)
    return (
        block_out,
        grad_input,
        grad_norm,
        vec_out[0],
        vec_out[1],
        vec_out[2],
        ada_out[0],
        ada_out[1],
        ada_out[2],
        qkv_out[0],
        qkv_out[1],
        qkv_out[2],
        attn_out[0],
        attn_out[1],
        attn_out[2],
        in_out[0],
        in_out[1],
        in_out[2],
        out_out[0],
        out_out[1],
        out_out[2],
    )


F32, BF = jnp.float32, jnp.bfloat16
MESH = pl.DeviceIdType.MESH
DP, LINE, SEQ, CHIPS, ALL = 4, 4, 8, 16, 32
ROWS, WIDTH, PACK = 128, 768, 640
HALF = WIDTH // 2
HALVES = ((0, 0), (0, 1), (0, 2), (2, 2), (1, 0), (1, 1), (1, 2), None, (2, 0), (2, 1))

def numbered(**counts):
    at = {}
    for name, count in counts.items():
        at[name] = sum(counts[other] for other in at)
    return SimpleNamespace(**at), sum(counts.values())


S, SEM_COUNT = numbered(
    cond=1,
    mix_qkv=1,
    mix_in=1,
    mix_attn=1,
    mod=1,
    w_qkv=1,
    w_attn=1,
    w_in=1,
    w_out=1,
    group_qkv=1,
    group_attn=1,
    fw_qkv=1,
    fw_attn=1,
    fw_in=1,
    fw_out=1,
    h1=4,
    h2=4,
    dm=4,
    xf=4,
    o=1,
    mm=1,
    dh2=1,
    do=1,
    gp=1,
    dh1=1,
    pair_out=1,
    pair_in=1,
    pair_attn=1,
    pair_qkv=1,
    plane_attn=1,
    plane_qkv=1,
    line_out=1,
    line_in=1,
    line_attn=1,
    line_qkv=1,
    last_in=1,
    last_attn=1,
    last_qkv=1,
    early=1,
    early2=1,
    late=1,
    late2=1,
    sq=1,
)

SCRATCH = dict(
    wide_qkv=((48, 3072), F32),
    wide_in=((48, 3072), F32),
    wide_attn=((48, 768), F32),
    s_qkv=((48, 3072), BF),
    s_in=((48, 3072), BF),
    s_attn=((48, 768), BF),
    s_out=((96, 768), BF),
    w_qkv=((768, 768), BF),
    w_in=((768, 768), BF),
    w_attn=((768, 768), BF),
    w_out=((4, 2, 96, 768), BF),
    conds_all=((4, 8, 128), F32),
    mod_send=((4, 4, 128), F32),
    mod_got=((32, 4, 128), F32),
    mod_flat=((40, 128), F32),
    mod_pad=((8, 384), F32),
    turn=((2, 4, 128, 128), F32),
    dmod_flat=((4, 40, 128), F32),
    mod=((8, 768), F32),
    x0=((128, 768), F32),
    n1=((128, 768), F32),
    inv1=((128, 128), F32),
    x1=((128, 768), F32),
    n2=((128, 768), F32),
    inv2=((128, 128), F32),
    a=((128, 768), F32),
    dx1=((128, 768), F32),
    h1=((4, 128, 768), BF),
    h2=((4, 128, 768), BF),
    dm=((4, 128, 768), BF),
    gb=((4, 128, 768), BF),
    du=((4, 128, 768), BF),
    xb=((2, 4, 128, 640), BF),
    pt=((3, 1024, 512), BF),
    ot=((2, 128, 512), F32),
    os=((4, 128, 256), BF),
    ob=((4, 128, 256), BF),
    mms=((4, 128, 768), BF),
    mmr=((4, 128, 768), BF),
    dhs=((4, 128, 768), BF),
    dhr=((4, 128, 768), BF),
    das=((128, 768), BF),
    dos=((4, 128, 256), BF),
    dob=((4, 128, 256), BF),
    dst=((3, 1024, 512), BF),
    ga=((512, 640), F32),
    gps=((512, 512), BF),
    gpr=((512, 512), BF),
    dqkv=((4, 128, 768), BF),
    d1s=((4, 128, 768), BF),
    d1r=((4, 128, 768), BF),
    g_out=((4, 2, 96, 768), BF),
    g_in=((2, 768, 384), BF),
    g_attn=((2, 768, 384), BF),
    g_qkv=((2, 768, 384), BF),
    p_out=((4, 96, 768), BF),
    p_in=((768, 384), BF),
    p_attn=((768, 384), BF),
    p_qkv=((768, 384), BF),
    q_attn=((4, 192, 384), BF),
    q_qkv=((4, 192, 384), BF),
    m_attn=((192, 384), BF),
    m_qkv=((192, 384), BF),
    r_out=((4, 96, 768), BF),
    r_in=((16, 48, 384), BF),
    r_attn=((4, 48, 384), BF),
    r_qkv=((4, 48, 384), BF),
    t_in=((4, 48, 384), F32),
    t_attn=((1, 48, 384), F32),
    t_qkv=((4, 48, 384), F32),
    f_in=((4, 2, 24, 384), F32),
    f_attn=((1, 2, 24, 384), F32),
    f_qkv=((4, 2, 24, 384), F32),
    early=((8, 768), F32),
    early_got=((8, 8, 768), F32),
    early_all=((4, 8, 768), F32),
    late=((4, 768), F32),
    late_got=((8, 4, 768), F32),
    late_all=((4, 4, 768), F32),
    sq=((32, 1, 128), F32),
)


def dot(left, right):
    return jnp.dot(left, right, preferred_element_type=F32)


def dot_nt(left, right):
    return lax.dot_general(left, right, (((1,), (1,)), ((), ())), preferred_element_type=F32)


def dot_tn(left, right):
    return lax.dot_general(left, right, (((0,), (0,)), ((), ())), preferred_element_type=F32)


def loop(count, body, start=0):
    def step(index, carry):
        body(index)
        return carry

    lax.fori_loop(start, count, step, 0)


def layer_kernel(
    i_time,
    i_start,
    i_len,
    i_tok,
    i_cot,
    i_vec,
    i_wada,
    i_wqkv,
    i_wattn,
    i_win,
    i_wout,
    o_y,
    o_dx,
    o_norm,
    o_gqkv,
    o_gattn,
    o_gin,
    o_gout,
    o_dmod,
    o_gvec,
    o_vec,
    o_conds,
    *scratch,
):
    r = SimpleNamespace(**dict(zip(SCRATCH, scratch)))
    send_sems, recv_sems = scratch[-2:]
    b, s = lax.axis_index("dp"), lax.axis_index("seq")
    z, c = lax.div(s, 2), lax.rem(s, 2)
    mate = s + 1 - 2 * c
    chip = b * LINE + z
    me = b * SEQ + s
    drains = []

    def push(src, dst, at, to_b, to_s):
        pltpu.make_async_remote_copy(
            src_ref=src,
            dst_ref=dst,
            send_sem=send_sems.at[at],
            recv_sem=recv_sems.at[at],
            device_id=(to_b, to_s),
            device_id_type=MESH,
        ).start()

    def keep(src, dst, at):
        pltpu.make_async_copy(src, dst, recv_sems.at[at]).start()

    def got(at, like):
        pltpu.make_async_copy(like, like, recv_sems.at[at]).wait()

    def left(at, like):
        pltpu.make_async_copy(like, like, send_sems.at[at]).wait()

    def sent(at, like):
        drains.append((at, like))

    def peers(body):
        for k in (1, 2, 3):
            body(lax.rem(b + k, DP))

    def stack(body):
        for k in (1, 2, 3):
            body(lax.rem(z + k, LINE))

    lane = lax.broadcasted_iota(jnp.int32, (1, 128), 1)
    low = lane < 64
    own24 = pl.ds(pl.multiple_of(24 * c, 8), 24)
    mate24 = pl.ds(pl.multiple_of(24 * (1 - c), 8), 24)
    part = pl.ds(pl.multiple_of(HALF * c, 128), HALF)
    chip_rows = pl.ds(pl.multiple_of(48 * chip, 16), 48)
    group_rows = pl.ds(pl.multiple_of(192 * b, 16), 192)

    barrier = pltpu.get_barrier_semaphore()

    def greet(k):
        other = lax.rem(me + k, ALL)
        pl.semaphore_signal(
            barrier, inc=1, device_id=(lax.div(other, SEQ), lax.rem(other, SEQ)), device_id_type=MESH
        )

    loop(ALL, greet, 1)

    def natural(kind, p, head):
        return kind * WIDTH + 192 * p + 64 * head

    def half_at(ref, column, high):
        tile = ref[:, column // 128 * 128 : column // 128 * 128 + 128]
        return tile if (column % 128 == 64) == high else pltpu.roll(tile, 64, 1)

    for p in range(4):
        for tile in range(5):
            pair = []
            for high in (0, 1):
                which = HALVES[2 * tile + high]
                pair.append(
                    jnp.zeros((24, 128), F32)
                    if which is None
                    else half_at(i_wqkv, natural(which[0], p, which[1]), bool(high))
                )
            r.wide_qkv[own24, 768 * p + 128 * tile : 768 * p + 128 * tile + 128] = jnp.where(
                low, pair[0], pair[1]
            )
        r.wide_qkv[own24, 768 * p + 640 : 768 * p + 768] = jnp.zeros((24, 128), F32)
    r.wide_in[own24, :] = i_win[...]
    r.wide_attn[own24, :] = i_wattn[...]
    r.s_out[...] = i_wout[...].astype(BF)
    lanes8 = lax.broadcasted_iota(jnp.int32, (8, 128), 1)
    half_cond = COND // 2
    speed = jnp.exp((lanes8 % half_cond).astype(F32) * (-math.log(10000.0) / half_cond))
    angle = i_time[0].astype(F32) * speed
    wave = jnp.where(lanes8 < half_cond, jnp.cos(angle), jnp.sin(angle))
    r.conds_all[b] = wave * (1.0 / (1.0 + jnp.exp(-wave)))
    pl.semaphore_wait(barrier, ALL - 1)

    def stack_rows(to):
        push(r.s_out, r.w_out.at[z, c], S.w_out, b, 2 * to + c)

    peers(lambda to: push(r.conds_all.at[b], r.conds_all.at[b], S.cond, to, s))
    sent(S.cond, r.conds_all.at[0:3])
    push(r.wide_qkv.at[own24], r.wide_qkv.at[own24], S.mix_qkv, b, mate)
    sent(S.mix_qkv, r.wide_qkv.at[0:24])
    push(r.wide_attn.at[own24], r.wide_attn.at[own24], S.mix_attn, b, mate)
    sent(S.mix_attn, r.wide_attn.at[0:24])
    push(r.wide_in.at[own24], r.wide_in.at[own24], S.mix_in, b, mate)
    sent(S.mix_in, r.wide_in.at[0:24])

    got(S.cond, r.conds_all.at[0:3])
    row8 = lax.broadcasted_iota(jnp.int32, (8, 128), 0)
    cond4 = jnp.zeros((8, 128), F32)
    for k in range(4):
        cond4 = jnp.where(row8 == k, r.conds_all[k], cond4)
    o_conds[...] = cond4
    wide = i_wada.shape[0]
    r.mod_pad[...] = jnp.zeros((8, 384), F32)
    r.mod_pad[:, 0:wide] = dot_nt(cond4.astype(BF), i_wada[...].astype(BF))
    columns = pltpu.roll(r.mod_pad[...], lax.rem(wide * me, 128), 1)
    for k in range(4):
        for t in range(3):
            r.mod_send[k, t : t + 1, :] = columns[k : k + 1, 128 * t : 128 * t + 128]
        r.mod_send[k, 3:4, :] = jnp.zeros((1, 128), F32)

    def send_mod(k):
        other = lax.rem(me + k, ALL)
        ob = lax.div(other, SEQ)
        push(r.mod_send.at[ob], r.mod_got.at[me], S.mod, ob, lax.rem(other, SEQ))

    loop(ALL, send_mod, 1)
    sent(S.mod, r.mod_got.at[0:31])
    keep(r.mod_send.at[b], r.mod_got.at[me], S.mod)

    def block(src, first):
        return src.at[:, pl.ds(pl.multiple_of(first, 128), HALF)]

    def spread(src, dst, at):
        def one(k):
            to = lax.rem(chip + k, CHIPS)
            to_b, to_z = lax.div(to, LINE), lax.rem(to, LINE)
            push(
                block(src, WIDTH * to_b + HALF * c),
                dst.at[chip_rows, part],
                at,
                to_b,
                2 * to_z + c,
            )

        loop(CHIPS, one, 1)
        keep(block(src, WIDTH * b + HALF * c), dst.at[chip_rows, part], at)
        sent(at, dst.at[0:720, 0:HALF])

    def along_line(src, dst, at, step):
        stack(
            lambda to: push(
                block(src, step * to + HALF * c), dst.at[chip_rows, part], at, b, 2 * to + c
            )
        )
        keep(block(src, step * z + HALF * c), dst.at[chip_rows, part], at)
        sent(at, dst.at[0:144, 0:HALF])

    def over_plane(dst, first, at):
        got(first, dst.at[0:192, 0:HALF])
        peers(
            lambda to: push(dst.at[group_rows, part], dst.at[group_rows, part], at, to, s)
        )
        sent(at, dst.at[0:576, 0:HALF])

    def share(dst, at, onward, rows):
        got(at, dst.at[0:rows, 0:HALF])
        push(dst.at[:, part], dst.at[:, part], onward, b, mate)
        sent(onward, dst.at[:, 0:HALF])

    got(S.mix_qkv, r.wide_qkv.at[0:24])
    r.s_qkv[...] = r.wide_qkv[...].astype(BF)
    along_line(r.s_qkv, r.w_qkv, S.w_qkv, WIDTH)
    got(S.mix_attn, r.wide_attn.at[0:24])
    r.s_attn[...] = r.wide_attn[...].astype(BF)
    along_line(r.s_attn, r.w_attn, S.w_attn, 0)

    place = s * ROWS + lax.broadcasted_iota(jnp.int32, (ROWS, 1), 0)
    hidden = (place >= i_start[0]) & (place < i_start[0] + i_len[0])
    x0 = jnp.where(hidden, i_vec[8:9, :], i_tok[0].astype(F32))
    r.x0[...] = x0
    n1, inv1 = normalize(x0)
    r.n1[...] = n1
    r.inv1[...] = jnp.broadcast_to(inv1, (ROWS, 128))

    got(S.mod, r.mod_got)
    r.mod_flat[...] = jnp.zeros((40, 128), F32)
    for k in range(ALL):
        first = 9 * k // 8
        r.mod_flat[first : first + 3, :] += r.mod_got[k, 0:3, :]
    for k in range(6):
        row = jnp.concatenate(
            [r.mod_flat[6 * k + t : 6 * k + t + 1, :] for t in range(6)], axis=1
        )
        r.mod[k : k + 1, :] = row + i_vec[2 + k : 3 + k, :]

    def mod(k):
        return r.mod[k : k + 1, :]

    def vec(k):
        return i_vec[k : k + 1, :]

    r.h1[z] = (r.n1[...] * vec(0) * (1.0 + mod(1)) + mod(0)).astype(BF)
    stack(lambda to: push(r.h1.at[z], r.h1.at[z], S.h1 + z, b, 2 * to + c))
    sent(S.h1 + z, r.h1.at[0:3])
    r.dm[b] = (i_cot[0].astype(F32) * mod(5)).astype(BF)
    over_plane(r.w_qkv, S.w_qkv, S.group_qkv)
    peers(lambda to: push(r.dm.at[b], r.dm.at[b], S.dm + b, to, s))
    sent(S.dm + b, r.dm.at[0:3])

    lanes = lax.broadcasted_iota(jnp.int32, (ROWS, 128), 1)
    first_half = lanes % HD < HD // 2
    speed = jnp.exp((lanes % (HD // 2)).astype(F32) * (-math.log(10000.0) / (HD // 2)))
    row = lax.broadcasted_iota(jnp.int32, (ROWS, 128), 0)

    def table(k):
        angle = ((2 * k + c) * ROWS + row).astype(F32) * speed
        r.turn[0, k] = jnp.cos(angle)
        sine = jnp.sin(angle)
        r.turn[1, k] = jnp.where(first_half, -sine, sine)

    loop(LINE, table)

    got(S.mix_in, r.wide_in.at[0:24])
    r.s_in[...] = r.wide_in[...].astype(BF)

    share(r.w_qkv, S.group_qkv, S.fw_qkv, 576)
    over_plane(r.w_attn, S.w_attn, S.group_attn)
    got(S.fw_qkv, r.w_qkv.at[:, 0:HALF])

    def turned(tile, sign, k):
        other = jnp.where(first_half, pltpu.roll(tile, 96, 1), pltpu.roll(tile, 32, 1))
        return tile * r.turn[0, k] + sign * (other * r.turn[1, k])

    def project(j):
        k = lax.rem(z + j, LINE)

        @pl.when(j > 0)
        def _():
            got(S.h1 + k, r.h1.at[0])

        x = dot(r.h1[k], r.w_qkv[:, 0:PACK])
        tiles = [x[:, 128 * t : 128 * t + 128] for t in range(5)]
        tiles[0] = turned(tiles[0], 1.0, k) * 0.125
        tiles[1] = jnp.where(low, turned(tiles[1], 1.0, k) * 0.125, tiles[1])
        tiles[2] = turned(tiles[2], 1.0, k)
        tiles[3] = turned(tiles[3], 1.0, k)
        for t in range(5):
            r.xb[0, k, :, 128 * t : 128 * t + 128] = tiles[t].astype(BF)
        push(r.xb.at[0, k], r.xb.at[1, k], S.xf + k, b, mate)

    loop(4, project)
    for k in range(4):
        sent(S.xf + k, r.xb.at[0, 0])

    stack(stack_rows)
    keep(r.s_out, r.w_out.at[z, c], S.w_out)
    sent(S.w_out, r.w_out.at[0:3, 0])
    spread(r.s_in, r.w_in, S.w_in)
    for k in range(4):
        got(S.xf + k, r.xb.at[0, 0])

    def tile_of(t):
        return r.xb[:, :, :, 128 * t : 128 * t + 128].reshape(1024, 128)

    heads = ((0, 2, 4, True, True), (0, 2, 4, False, False), (1, 3, 1, True, False))

    def queries(head, first, size):
        q_tile, _, _, q_low, _ = heads[head]
        q = r.xb[0, first : first + size, :, 128 * q_tile : 128 * q_tile + 128]
        return jnp.where(low if q_low else ~low, q.reshape(size * 128, 128), jnp.zeros((), BF))

    for half in range(2):
        at = slice(256 * half, 256 * half + 256)
        for head in range(3):
            scores = dot_nt(tile_of(heads[head][1]), queries(head, 2 * half, 2))
            weights = jnp.exp(scores - jnp.max(scores, axis=0, keepdims=True))
            weights = weights * (1.0 / jnp.sum(weights, axis=0, keepdims=True))
            weights = weights.astype(BF)
            r.pt[head, :, at] = weights
            out = dot_tn(tile_of(heads[head][2]), weights)
            if head == 0:
                r.ot[0, 0:64, at] = out[0:64]
            elif head == 1:
                r.ot[0, 64:128, at] = out[64:128]
            else:
                r.ot[1, 0:64, at] = out[64:128]
                r.ot[1, 64:128, at] = jnp.zeros((64, 256), F32)
        for t in range(2):
            r.os[2 * half : 2 * half + 2, :, 128 * t : 128 * t + 128] = (
                r.ot[t, :, at].T.astype(BF).reshape(2, 128, 128)
            )
        for to in (2 * half, 2 * half + 1):

            @pl.when(z == to)
            def _():
                keep(r.os.at[to], r.ob.at[z], S.o)

            @pl.when(z != to)
            def _():
                push(r.os.at[to], r.ob.at[z], S.o, b, 2 * to + c)

    sent(S.o, r.os.at[0:3])
    share(r.w_attn, S.group_attn, S.fw_attn, 576)
    got(S.fw_attn, r.w_attn.at[:, 0:HALF])
    got(S.o, r.ob)
    a = jnp.zeros((ROWS, WIDTH), F32)
    for p in range(4):
        a += dot(r.ob[p, :, 0:128], r.w_attn[192 * p : 192 * p + 128, :])
        a += dot(r.ob[p, :, 128:192], r.w_attn[192 * p + 128 : 192 * p + 192, :])
    r.a[...] = a
    x1 = r.x0[...] + mod(2) * a
    r.x1[...] = x1
    n2, inv2 = normalize(x1)
    r.n2[...] = n2
    r.inv2[...] = jnp.broadcast_to(inv2, (ROWS, 128))
    r.h2[b] = (n2 * vec(1) * (1.0 + mod(4)) + mod(3)).astype(BF)
    peers(lambda to: push(r.h2.at[b], r.h2.at[b], S.h2 + b, to, s))
    sent(S.h2 + b, r.h2.at[0:3])
    got(S.w_out, r.w_out.at[:, 0])
    push(r.w_out.at[:, c], r.w_out.at[:, c], S.fw_out, b, mate)
    sent(S.fw_out, r.w_out.at[:, 0])
    share(r.w_in, S.w_in, S.fw_in, 768)
    got(S.fw_out, r.w_out.at[:, 0])
    got(S.fw_in, r.w_in.at[:, 0:HALF])

    def feed(j):
        k = lax.rem(b + j, DP)

        @pl.when(j > 0)
        def _():
            got(S.h2 + k, r.h2.at[0])
            got(S.dm + k, r.dm.at[0])

        u = dot(r.h2[k], r.w_in[...])
        slope = 0.7978845608028654
        cube = 0.044715
        t = jnp.tanh(slope * (u + cube * u * u * u))
        r.gb[k] = (0.5 * u * (1.0 + t)).astype(BF)
        bend = 0.5 * (1.0 + t) + 0.5 * u * (1.0 - t * t) * (slope * (1.0 + 3.0 * cube * u * u))
        r.du[k] = (dot_nt(r.dm[k], r.w_out[...].reshape(768, 768)) * bend).astype(BF)
        r.dhs[k] = dot_nt(r.du[k], r.w_in[...]).astype(BF)

        @pl.when(j > 0)
        def _():
            push(r.dhs.at[k], r.dhr.at[b], S.dh2, k, s)

    loop(4, feed)
    sent(S.dh2, r.dhs.at[0:3])

    def feed_out(j):
        k = lax.rem(b + j, DP)
        r.mms[k] = dot(r.gb[k], r.w_out[...].reshape(768, 768)).astype(BF)

        @pl.when(j > 0)
        def _():
            push(r.mms.at[k], r.mmr.at[b], S.mm, k, s)

    loop(4, feed_out)
    sent(S.mm, r.mms.at[0:3])

    def gather(own, others):
        total = own[b].astype(F32)
        for k in (1, 2, 3):
            total += others[lax.rem(b + k, DP)].astype(F32)
        return total

    for k in range(4):
        rows = slice(192 * k, 192 * k + 192)
        block = dot_tn(r.gb[:, :, rows].reshape(512, 192), r.dm[...].reshape(512, 768))
        r.g_out[k] = block.astype(BF).reshape(2, 96, 768)
    push(r.g_out.at[:, 1 - c], r.p_out, S.pair_out, b, mate)
    sent(S.pair_out, r.p_out)

    def outer(left, right, dst):
        def one(k):
            rows = pl.ds(pl.multiple_of(128 * k, 128), 128)
            result = dot_tn(
                left[:, :, rows].reshape(512, 128), right[...].reshape(512, 768)
            ).astype(BF)
            dst[0, rows, :] = result[:, 0:HALF]
            dst[1, rows, :] = result[:, HALF:WIDTH]

        loop(6, one)

    def to_mate(grad, dst, at):
        push(grad.at[1 - c], dst, at, b, mate)
        sent(at, dst)

    def pair_sum(grad, pair, at):
        got(at, pair)
        grad[c] = (grad[c].astype(F32) + pair[...].astype(F32)).astype(BF)

    def plane_sum(grad, dst, at):
        def rows(to):
            return grad.at[c, pl.ds(pl.multiple_of(192 * to, 16), 192)]

        peers(lambda to: push(rows(to), dst.at[b], at, to, s))
        keep(rows(b), dst.at[b], at)
        sent(at, dst.at[0:3])

    def line_sum(src, total, dst, first, at):
        got(first, src)
        total[...] = (
            (src[0].astype(F32) + src[1].astype(F32)) + (src[2].astype(F32) + src[3].astype(F32))
        ).astype(BF)

        def rows(to):
            return total.at[pl.ds(pl.multiple_of(48 * to, 16), 48)]

        stack(lambda to: push(rows(to), dst.at[z], at, b, 2 * to + c))
        keep(rows(z), dst.at[z], at)
        sent(at, dst.at[0:3])

    def trade(total, final, at):
        push(total.at[:, mate24], final.at[:, c], at, b, mate)
        sent(at, final.at[:, 0])
        final[:, c] = total[:, own24, :]

    outer(r.h2, r.du, r.g_in)
    to_mate(r.g_in, r.p_in, S.pair_in)

    got(S.pair_out, r.p_out)
    for k in range(4):
        r.g_out[k, c] = (r.g_out[k, c].astype(F32) + r.p_out[k].astype(F32)).astype(BF)

    def send_gout(to):
        push(r.g_out.at[to, c], r.r_out.at[z], S.line_out, b, 2 * to + c)

    stack(send_gout)
    keep(r.g_out.at[z, c], r.r_out.at[z], S.line_out)
    sent(S.line_out, r.r_out.at[0:3])

    got(S.dh2, r.dhr.at[0:3])
    dh = gather(r.dhs, r.dhr)
    n2 = r.n2[...]
    inv2 = r.inv2[:, 0:1]
    r.early[...] = jnp.zeros((8, 768), F32)
    r.early[2:3, :] = jnp.sum(dh, axis=0, keepdims=True)
    both = jnp.sum(dh * n2, axis=0, keepdims=True)
    r.early[3:4, :] = both * vec(1)
    r.early[0:1, :] = both * (1.0 + mod(4))
    grad = dh * ((1.0 + mod(4)) * vec(1))
    dx1 = i_cot[0].astype(F32) + norm_back(n2, inv2, grad)
    r.dx1[...] = dx1
    r.early[1:2, :] = jnp.sum(dx1 * r.a[...], axis=0, keepdims=True)
    r.das[...] = (dx1 * mod(2)).astype(BF)
    for p in range(4):
        first = 192 * p
        r.dos[p, :, 0:128] = dot_nt(r.das[...], r.w_attn[first : first + 128, :]).astype(BF)
        tail = dot_nt(r.das[...], r.w_attn[first + 128 : first + 192, :])
        r.dos[p, :, 128:256] = jnp.concatenate(
            [tail, jnp.zeros((ROWS, 64), F32)], axis=1
        ).astype(BF)

    stack(lambda to: push(r.dos.at[to], r.dob.at[z], S.do, b, 2 * to + c))
    keep(r.dos.at[z], r.dob.at[z], S.do)
    sent(S.do, r.dos.at[0:3])

    for p in range(4):
        rows = slice(192 * p, 192 * p + 192)
        result = dot_tn(r.ob[p], r.das[...])[0:192].astype(BF)
        r.g_attn[0, rows, :] = result[:, 0:HALF]
        r.g_attn[1, rows, :] = result[:, HALF:WIDTH]
    to_mate(r.g_attn, r.p_attn, S.pair_attn)

    got(S.mm, r.mmr.at[0:3])
    mm = gather(r.mms, r.mmr)
    o_y[...] = (r.x1[...] + mod(5) * mm).astype(BF)
    r.early[4:5, :] = jnp.sum(i_cot[0].astype(F32) * mm, axis=0, keepdims=True)

    def over_line(src, dst, name):
        def one(k):
            push(src, dst.at[s], name, b, lax.rem(s + k, SEQ))

        loop(SEQ, one, 1)
        keep(src, dst.at[s], name)
        sent(name, dst.at[0:7])

    def over_group(got_ref, dst, name):
        total = got_ref[0]
        for k in range(1, SEQ):
            total += got_ref[k]
        dst[b] = total
        peers(lambda to: push(dst.at[b], dst.at[b], name, to, s))
        sent(name, dst.at[0:3])

    over_line(r.early, r.early_got, S.early)

    pair_sum(r.g_in, r.p_in, S.pair_in)

    def send_gin(k):
        to = lax.rem(chip + k, CHIPS)
        push(
            r.g_in.at[c, pl.ds(pl.multiple_of(48 * to, 16), 48)],
            r.r_in.at[chip],
            S.line_in,
            lax.div(to, LINE),
            2 * lax.rem(to, LINE) + c,
        )

    loop(CHIPS, send_gin, 1)
    keep(r.g_in.at[c, chip_rows], r.r_in.at[chip], S.line_in)
    sent(S.line_in, r.r_in.at[0:15])
    pair_sum(r.g_attn, r.p_attn, S.pair_attn)
    plane_sum(r.g_attn, r.q_attn, S.plane_attn)

    got(S.do, r.dob)
    dot0, dot1 = r.dob[:, :, 0:128].reshape(512, 128), r.dob[:, :, 128:256].reshape(512, 128)
    zero = jnp.zeros((), BF)
    moved = pltpu.roll(dot1.astype(F32), 64, 1).astype(BF)
    grads = (jnp.where(low, dot0, zero), jnp.where(low, zero, dot0), moved)
    product = dot0.astype(F32).T * r.ot[0]
    deltas = (
        jnp.sum(product[0:64], axis=0, keepdims=True),
        jnp.sum(product[64:128], axis=0, keepdims=True),
        jnp.sum(dot1.astype(F32).T * r.ot[1], axis=0, keepdims=True),
    )
    for head in range(3):
        values = tile_of(heads[head][2])
        for half in range(2):
            at = slice(256 * half, 256 * half + 256)
            dp = dot_nt(values, grads[head][at])
            r.dst[head, :, at] = (
                r.pt[head, :, at].astype(F32) * (dp - deltas[head][:, at])
            ).astype(BF)

    def key_grads(rows):
        dk = [dot(r.dst[head, rows, :], queries(head, 0, 4)) for head in range(3)]
        dv = [dot(r.pt[head, rows, :], grads[head]) for head in range(3)]
        return (dv[2], dk[0] + dk[1], dk[2], dv[0] + dv[1])

    for t, tile in enumerate(key_grads(slice(512, 1024))):
        r.gps[:, 128 * t : 128 * t + 128] = tile.astype(BF)
    push(r.gps, r.gpr, S.gp, b, mate)
    sent(S.gp, r.gps)
    for t, tile in enumerate(key_grads(slice(0, 512))):
        r.ga[:, 128 * t + 128 : 128 * t + 256] = tile
    for half in range(2):
        at = slice(256 * half, 256 * half + 256)
        turned_q = [dot_tn(tile_of(heads[head][1]), r.dst[head, :, at]) for head in range(3)]
        top = jnp.concatenate([turned_q[0][0:64], turned_q[1][64:128]], axis=0)
        r.ga[at, 0:128] = top.T * 0.125
        r.ga[at, 128:256] += turned_q[2].T * 0.125
    got(S.gp, r.gpr)

    def unproject(j):
        k = lax.rem(z + 1 + j, LINE)
        rows = pl.ds(pl.multiple_of(128 * k, 128), 128)
        tiles = [r.ga[rows, 0:128]] + [
            r.ga[rows, 128 * t : 128 * t + 128]
            + r.gpr[rows, 128 * t - 128 : 128 * t].astype(F32)
            for t in range(1, 5)
        ]
        tiles[0] = turned(tiles[0], -1.0, k)
        tiles[1] = jnp.where(low, turned(tiles[1], -1.0, k), tiles[1])
        tiles[2] = turned(tiles[2], -1.0, k)
        tiles[3] = turned(tiles[3], -1.0, k)
        for t in range(5):
            r.dqkv[k, :, 128 * t : 128 * t + 128] = tiles[t].astype(BF)
        r.dqkv[k, :, PACK:WIDTH] = jnp.zeros((128, 128), BF)
        r.d1s[k] = dot_nt(r.dqkv[k, :, 0:PACK], r.w_qkv[:, 0:PACK]).astype(BF)

        @pl.when(j < 3)
        def _():
            push(r.d1s.at[k], r.d1r.at[z], S.dh1, b, 2 * k + c)

    loop(4, unproject)
    sent(S.dh1, r.d1s.at[0:3])
    outer(r.h1, r.dqkv, r.g_qkv)
    to_mate(r.g_qkv, r.p_qkv, S.pair_qkv)
    line_sum(r.q_attn, r.m_attn, r.r_attn, S.plane_attn, S.line_attn)
    got(S.early, r.early_got)
    over_group(r.early_got, r.early_all, S.early2)
    pair_sum(r.g_qkv, r.p_qkv, S.pair_qkv)
    plane_sum(r.g_qkv, r.q_qkv, S.plane_qkv)

    got(S.line_in, r.r_in)
    for p in range(4):
        r.t_in[p] = (r.r_in[4 * p].astype(F32) + r.r_in[4 * p + 1].astype(F32)) + (
            r.r_in[4 * p + 2].astype(F32) + r.r_in[4 * p + 3].astype(F32)
        )
    trade(r.t_in, r.f_in, S.last_in)
    line_sum(r.q_qkv, r.m_qkv, r.r_qkv, S.plane_qkv, S.line_qkv)

    got(S.dh1, r.d1r.at[0:3])
    dh = r.d1s[z].astype(F32)
    for k in (1, 2, 3):
        dh += r.d1r[lax.rem(z + k, LINE)].astype(F32)
    n1 = r.n1[...]
    both = jnp.sum(dh * n1, axis=0, keepdims=True)
    r.late[0:1, :] = both * (1.0 + mod(1))
    r.late[1:2, :] = jnp.sum(dh, axis=0, keepdims=True)
    r.late[2:3, :] = both * vec(0)
    grad = dh * ((1.0 + mod(1)) * vec(0))
    dx0 = r.dx1[...] + norm_back(n1, r.inv1[:, 0:1], grad)
    o_dx[...] = jnp.where(hidden, 0.0, dx0)
    r.late[3:4, :] = jnp.sum(jnp.where(hidden, dx0, 0.0), axis=0, keepdims=True)
    over_line(r.late, r.late_got, S.late)

    got(S.line_out, r.r_out)
    total = (r.r_out[0].astype(F32) + r.r_out[1].astype(F32)) + (
        r.r_out[2].astype(F32) + r.r_out[3].astype(F32)
    )
    o_gout[...] = total
    squares = total * total
    squares = jnp.sum(squares[:, 0:128] + squares[:, 128:256] + squares[:, 256:384]
                      + squares[:, 384:512] + squares[:, 512:640] + squares[:, 640:768],
                      axis=0, keepdims=True)

    def fold(value):
        total = value[:, 0:128] * value[:, 0:128]
        for t in range(1, value.shape[1] // 128):
            total += value[:, 128 * t : 128 * t + 128] * value[:, 128 * t : 128 * t + 128]
        return jnp.sum(total, axis=0, keepdims=True)

    got(S.line_attn, r.r_attn)
    r.t_attn[0] = (r.r_attn[0].astype(F32) + r.r_attn[1].astype(F32)) + (
        r.r_attn[2].astype(F32) + r.r_attn[3].astype(F32)
    )
    trade(r.t_attn, r.f_attn, S.last_attn)
    got(S.line_qkv, r.r_qkv)
    r.t_qkv[...] = r.r_qkv[...].astype(F32)
    trade(r.t_qkv, r.f_qkv, S.last_qkv)
    got(S.late, r.late_got)
    over_group(r.late_got, r.late_all, S.late2)
    got(S.last_in, r.f_in.at[:, 0])
    got(S.last_attn, r.f_attn.at[:, 0])
    for h in range(2):
        for p in range(4):
            value = r.f_in[p, h]
            o_gin[:, 768 * p + 384 * h : 768 * p + 384 * h + 384] = value
            squares += fold(value)
        value = r.f_attn[0, h]
        o_gattn[:, 384 * h : 384 * h + 384] = value
        squares += fold(value)
    got(S.last_qkv, r.f_qkv.at[:, 0])
    where = {which: index for index, which in enumerate(HALVES) if which is not None}

    def packed_half(chunk, high):
        kind, rest = chunk // 12, chunk % 12
        index = where[(kind, rest % 3)]
        t = index // 2
        tile = r.f_qkv[rest // 3, t // 3, :, t % 3 * 128 : t % 3 * 128 + 128]
        return tile if index % 2 == high else pltpu.roll(tile, 64, 1)

    for t in range(18):
        o_gqkv[:, 128 * t : 128 * t + 128] = jnp.where(
            low, packed_half(2 * t, 0), packed_half(2 * t + 1, 1)
        )
    for p in range(4):
        for h in range(2):
            squares += fold(r.f_qkv[p, h])

    r.sq[me] = squares

    def send_sq(k):
        other = lax.rem(me + k, ALL)
        push(r.sq.at[me], r.sq.at[me], S.sq, lax.div(other, SEQ), lax.rem(other, SEQ))

    loop(ALL, send_sq, 1)
    sent(S.sq, r.sq.at[0:31])
    got(S.early2, r.early_all.at[0:3])
    got(S.late2, r.late_all.at[0:3])
    mods = []
    for k in range(4):
        early, late = r.early_all[k], r.late_all[k]
        rows = jnp.concatenate([late[1:3], early[1:5], jnp.zeros((2, 768), F32)], axis=0)
        for n in range(6):
            for m in range(6):
                r.dmod_flat[k, 6 * n + m : 6 * n + m + 1, :] = rows[
                    n : n + 1, 128 * m : 128 * m + 128
                ]
        mods.append(rows)
    gain = jnp.concatenate(
        [
            sum(r.late_all[k][0:1] for k in range(4)),
            sum(r.early_all[k][0:1] for k in range(4)),
            (mods[0] + mods[1] + mods[2] + mods[3])[0:6],
        ],
        axis=0,
    )
    mask_row = sum(r.late_all[k][3:4] for k in range(4))
    gains = jnp.concatenate([gain, mask_row, jnp.zeros((7, 768), F32)], axis=0)
    masters = jnp.concatenate([i_vec[...], jnp.zeros((7, 768), F32)], axis=0)
    own = lax.rem(WIDTH - 24 * me, WIDTH)
    o_gvec[...] = pltpu.roll(gains, own, 1)[:, 0:128]
    o_vec[...] = pltpu.roll(masters, own, 1)[:, 0:128]
    r.mod_pad[...] = jnp.zeros((8, 384), F32)
    window = lax.div(wide * me, 128)
    for k in range(4):
        rows = r.dmod_flat[k, pl.ds(window, 3), :]
        for m in range(3):
            r.mod_pad[k : k + 1, 128 * m : 128 * m + 128] = rows[m : m + 1, :]
    o_dmod[...] = pltpu.roll(r.mod_pad[...], lax.rem(384 - lax.rem(wide * me, 128), 384), 1)[:, 0:256]
    small = jnp.sum(gain * gain) + jnp.sum(mask_row * mask_row)
    conds = [r.conds_all[k][0:1].astype(BF).astype(F32) for k in range(4)]
    for k in range(4):
        for m in range(k, 4):
            term = jnp.sum(mods[k] * mods[m]) * jnp.sum(conds[k] * conds[m])
            small += term if m == k else 2.0 * term
    got(S.sq, r.sq.at[0:31])
    total = r.sq[0]
    for k in range(1, ALL):
        total += r.sq[k]
    o_norm[...] = jnp.broadcast_to(jnp.sqrt(jnp.sum(total) + small), (8, 128))

    for at, like in drains:
        left(at, like)


def run_layer(*args):
    shapes = (
        ((ROWS, WIDTH), BF),
        ((ROWS, WIDTH), F32),
        ((8, 128), F32),
        ((24, 3 * WIDTH), F32),
        ((24, WIDTH), F32),
        ((24, 4 * WIDTH), F32),
        ((96, WIDTH), F32),
        ((8, 256), F32),
        ((16, 128), F32),
        ((16, 128), F32),
        ((8, 128), F32),
    )
    whole = pl.BlockSpec(memory_space=pltpu.VMEM)
    scalar = pl.BlockSpec(memory_space=pltpu.SMEM)
    return pl.pallas_call(
        layer_kernel,
        out_shape=[jax.ShapeDtypeStruct(shape, kind) for shape, kind in shapes],
        in_specs=[scalar] * 3 + [whole] * (len(args) - 3),
        out_specs=[whole] * len(shapes),
        scratch_shapes=[pltpu.VMEM(shape, kind) for shape, kind in SCRATCH.values()]
        + [pltpu.SemaphoreType.DMA((SEM_COUNT,)), pltpu.SemaphoreType.DMA((SEM_COUNT,))],
        compiler_params=pltpu.CompilerParams(
            collective_id=0, has_side_effects=True, vmem_limit_bytes=60 * 1024 * 1024
        ),
    )(*args)


def finish_kernel(
    y, dx, norm, g_qkv, g_attn, g_in, g_out, dmod, g_vec, own_vec, conds, *rest
):
    (w_ada, w_qkv, w_attn, w_in, w_out), moments, outs = rest[:5], rest[5:17], rest[17:]
    outs[0][0] = y[...]
    outs[1][0] = dx[...]
    outs[2][0, 0] = norm[0, 0]
    clip = jnp.minimum(1.0, CLIP / (norm[0:1, 0:1] + 1e-06))
    columns = w_ada.shape[0]
    rounded = conds[...].astype(BF).astype(F32)
    turned_mod = dmod[...].T
    g_ada = turned_mod[0:columns, 0:1] * rounded[0:1, :]
    for k in range(1, 4):
        g_ada += turned_mod[0:columns, k : k + 1] * rounded[k : k + 1, :]
    narrow = moments[0].shape[1]
    grads = (
        g_vec[0:9, 0:narrow],
        g_ada,
        g_qkv[...],
        g_attn[...],
        g_in[...],
        g_out[...],
    )
    weights = (
        own_vec[0:9, 0:narrow],
        w_ada[...],
        w_qkv[...],
        w_attn[...],
        w_in[...],
        w_out[...],
    )
    for k in range(6):
        results = adam_step(
            weights[k],
            grads[k] * clip,
            moments[2 * k][...],
            moments[2 * k + 1][...],
            RATE if k else RATE_VECTORS,
            DECAY if k else 0.0,
        )
        for n in range(3):
            outs[3 + 3 * k + n][...] = results[n]


def run_finish(partial_results, weights, moments):
    shapes = [((1, ROWS, WIDTH), BF), ((1, ROWS, WIDTH), F32), ((1, 1), F32)]
    for moment in moments[::2]:
        shapes += [(moment.shape, F32)] * 3
    whole = pl.BlockSpec(memory_space=pltpu.VMEM)
    specs = [whole] * len(shapes)
    specs[2] = pl.BlockSpec(memory_space=pltpu.SMEM)
    args = (*partial_results, *weights, *moments)
    return pl.pallas_call(
        finish_kernel,
        out_shape=[jax.ShapeDtypeStruct(shape, kind) for shape, kind in shapes],
        in_specs=[whole] * len(args),
        out_specs=specs,
        compiler_params=pltpu.CompilerParams(vmem_limit_bytes=60 * 1024 * 1024),
    )(*args)


def slices(
    tokens_in,
    cotangent,
    timesteps,
    span_start,
    span_len,
    vectors,
    w_ada,
    w_qkv,
    w_attn,
    w_in,
    w_out,
    m_vec,
    v_vec,
    m_ada,
    v_ada,
    m_qkv,
    v_qkv,
    m_attn,
    v_attn,
    m_in,
    v_in,
    m_out,
    v_out,
):
    partial_results = run_layer(
        timesteps,
        span_start,
        span_len,
        tokens_in,
        cotangent,
        vectors,
        w_ada.T,
        w_qkv,
        w_attn,
        w_in,
        w_out,
    )
    moments = (
        m_vec,
        v_vec,
        m_ada.T,
        v_ada.T,
        m_qkv,
        v_qkv,
        m_attn,
        v_attn,
        m_in,
        v_in,
        m_out,
        v_out,
    )
    results = run_finish(partial_results, (w_ada.T, w_qkv, w_attn, w_in, w_out), moments)
    ada_results = [result.T for result in results[6:9]]
    return (*results[:2], results[2].reshape(()), *results[3:6], *ada_results, *results[9:])


def solution(mesh):
    in_specs = (
        P("dp", "seq", None),
        P("dp", "seq", None),
        P("dp"),
        P("dp"),
        P("dp"),
        P(),
        P(None, ("dp", "seq")),
        P(("dp", "seq"), None),
        P(("dp", "seq"), None),
        P(("dp", "seq"), None),
        P(("dp", "seq"), None),
        P(None, ("dp", "seq")),
        P(None, ("dp", "seq")),
        P(None, ("dp", "seq")),
        P(None, ("dp", "seq")),
        P(("dp", "seq"), None),
        P(("dp", "seq"), None),
        P(("dp", "seq"), None),
        P(("dp", "seq"), None),
        P(("dp", "seq"), None),
        P(("dp", "seq"), None),
        P(("dp", "seq"), None),
        P(("dp", "seq"), None),
    )
    out_specs = (
        P("dp", "seq", None),
        P("dp", "seq", None),
        P(),
        P(None, ("dp", "seq")),
        P(None, ("dp", "seq")),
        P(None, ("dp", "seq")),
        P(None, ("dp", "seq")),
        P(None, ("dp", "seq")),
        P(None, ("dp", "seq")),
        P(("dp", "seq"), None),
        P(("dp", "seq"), None),
        P(("dp", "seq"), None),
        P(("dp", "seq"), None),
        P(("dp", "seq"), None),
        P(("dp", "seq"), None),
        P(("dp", "seq"), None),
        P(("dp", "seq"), None),
        P(("dp", "seq"), None),
        P(("dp", "seq"), None),
        P(("dp", "seq"), None),
        P(("dp", "seq"), None),
    )
    sizes = dict(mesh.shape)
    local = slices if (sizes["dp"], sizes["seq"]) == (4, 8) else plain
    return jax.shard_map(local, mesh=mesh, in_specs=in_specs, out_specs=out_specs, check_vma=False)
```

```python
from functools import partial
import math
from types import SimpleNamespace

import jax
import jax.numpy as jnp
from jax import lax
from jax.experimental import pallas as pl
from jax.experimental.pallas import tpu as pltpu
from jax.sharding import PartitionSpec as P

HD = 64
COND = 128
STEP = 10


BETA_ONE = 0.9
BETA_TWO = 0.999
ADAM_EPS = 1e-08
RATE = 0.1
RATE_VECTORS = 0.3
DECAY = 0.01
CLIP = 1.0
NORM_EPS = 1e-05


def cond_input(timesteps):
    half_cond = COND // 2
    freqs = jnp.exp(jnp.arange(half_cond, dtype=jnp.float32) * (-math.log(10000.0) / half_cond))
    angles = timesteps.astype(jnp.float32)[:, None] * freqs[None, :]
    return jax.nn.silu(jnp.concatenate([jnp.cos(angles), jnp.sin(angles)], axis=1))


def rotary_tables(positions):
    half_head = HD // 2
    inverse = jnp.exp(jnp.arange(half_head, dtype=jnp.float32) * (-math.log(10000.0) / half_head))
    angles = positions.astype(jnp.float32)[:, None] * inverse[None, :]
    return (jnp.cos(angles), jnp.sin(angles))


def rotate(values, cosines, sines):
    half_head = values.shape[-1] // 2
    first = values[..., :half_head]
    second = values[..., half_head:]
    cos_b = cosines[:, None, :]
    sin_b = sines[:, None, :]
    return jnp.concatenate(
        [first * cos_b - second * sin_b, second * cos_b + first * sin_b], axis=-1
    )


def rotate_back(grads, cosines, sines):
    half_head = grads.shape[-1] // 2
    first = grads[..., :half_head]
    second = grads[..., half_head:]
    cos_b = cosines[:, None, :]
    sin_b = sines[:, None, :]
    return jnp.concatenate(
        [first * cos_b + second * sin_b, second * cos_b - first * sin_b], axis=-1
    )


def normalize(values):
    centre = jnp.mean(values, axis=-1, keepdims=True)
    centred = values - centre
    inverse = lax.rsqrt(jnp.mean(centred * centred, axis=-1, keepdims=True) + NORM_EPS)
    return (centred * inverse, inverse)


def norm_back(normed, inverse, grad):
    return inverse * (
        grad
        - jnp.mean(grad, axis=-1, keepdims=True)
        - normed * jnp.mean(grad * normed, axis=-1, keepdims=True)
    )


def split_kv(block, width):
    seqs, block_rows = (block.shape[0], block.shape[1])
    keys = block[..., :width].reshape(seqs, block_rows, width // HD, HD)
    values = block[..., width:].reshape(seqs, block_rows, width // HD, HD)
    return (keys, values)


def attend_piece(carry, piece, queries, width, factor):
    piece_rows = piece.shape[1]
    size = math.gcd(piece_rows, 512)

    def attend_one_block(index, state):
        running, denom, accum = state
        block = lax.dynamic_slice_in_dim(piece, index * size, size, 1)
        keys, values = split_kv(block, width)
        scores = (
            jnp.einsum("sqhd,skhd->shqk", queries, keys, preferred_element_type=jnp.float32)
            * factor
        )
        highest = jnp.maximum(running, jnp.max(scores, axis=-1))
        shrink = jnp.exp(running - highest)
        weights = jnp.exp(scores - highest[..., None])
        denom = denom * shrink + jnp.sum(weights, axis=-1)
        accum = accum * shrink[..., None] + jnp.einsum(
            "shqk,skhd->shqd",
            weights.astype(jnp.bfloat16),
            values,
            preferred_element_type=jnp.float32,
        )
        return (highest, denom, accum)

    return lax.fori_loop(0, piece_rows // size, attend_one_block, carry)


def block_grads(block, queries, grad_out, logsum, delta, width, factor):
    keys, values = split_kv(block, width)
    scores = (
        jnp.einsum("sqhd,skhd->shqk", queries, keys, preferred_element_type=jnp.float32) * factor
    )
    probs = jnp.exp(scores - logsum[..., None])
    dprobs = jnp.einsum("sqhd,skhd->shqk", grad_out, values, preferred_element_type=jnp.float32)
    dscores = (probs * (dprobs - delta[..., None])).astype(jnp.bfloat16)
    return (keys, probs, dscores)


def query_grads(kv_all, queries, grad_out, logsum, delta, width, factor):
    total_rows = kv_all.shape[1]
    size = math.gcd(total_rows, 512)

    def query_one_block(index, accum):
        block = lax.dynamic_slice_in_dim(kv_all, index * size, size, 1)
        keys, probs, dscores = block_grads(block, queries, grad_out, logsum, delta, width, factor)
        return accum + factor * jnp.einsum(
            "shqk,skhd->sqhd", dscores, keys, preferred_element_type=jnp.float32
        )

    return lax.fori_loop(
        0, total_rows // size, query_one_block, jnp.zeros(queries.shape, jnp.float32)
    )


def key_grads(kv_all, queries, grad_out, logsum, delta, width, factor, count):
    size = math.gcd(count, 512)
    seqs = queries.shape[0]

    def key_one_block(index, accum):
        block = lax.dynamic_slice_in_dim(kv_all, index * size, size, 1)
        keys, probs, dscores = block_grads(block, queries, grad_out, logsum, delta, width, factor)
        grad_vals = jnp.einsum(
            "shqk,sqhd->skhd",
            probs.astype(jnp.bfloat16),
            grad_out,
            preferred_element_type=jnp.float32,
        )
        grad_keys = factor * jnp.einsum(
            "shqk,sqhd->skhd", dscores, queries, preferred_element_type=jnp.float32
        )
        joined = jnp.concatenate(
            [grad_keys.reshape(seqs, size, width), grad_vals.reshape(seqs, size, width)], axis=-1
        )
        return lax.dynamic_update_slice_in_dim(
            accum, jnp.transpose(joined, (1, 0, 2)), index * size, 0
        )

    initial = jnp.zeros((count, seqs, 2 * width), jnp.float32)
    return lax.fori_loop(0, count // size, key_one_block, initial)


def adam_step(weight, grad, first, second, rate, decay_rate):
    new_first = BETA_ONE * first + (1.0 - BETA_ONE) * grad
    new_second = BETA_TWO * second + (1.0 - BETA_TWO) * grad * grad
    fixed_first = new_first / (1.0 - BETA_ONE**STEP)
    fixed_second = new_second / (1.0 - BETA_TWO**STEP)
    new_weight = weight - rate * (
        fixed_first / (jnp.sqrt(fixed_second) + ADAM_EPS) + decay_rate * weight
    )
    return (new_first, new_second, new_weight)


def mod_back(grad_hidden, ln_values, normed, scale_part, gain):
    grad_shift = jnp.sum(grad_hidden, axis=1)
    grad_scale = jnp.sum(grad_hidden * ln_values, axis=1)
    grad_ln = grad_hidden * (1.0 + scale_part)
    grad_gain = jnp.sum(grad_ln * normed, axis=(0, 1))
    return (grad_shift, grad_scale, grad_gain, grad_ln * gain)


def plain(
    tokens_in,
    cotangent,
    timesteps,
    span_start,
    span_len,
    vectors,
    w_ada,
    w_qkv,
    w_attn,
    w_in,
    w_out,
    m_vec,
    v_vec,
    m_ada,
    v_ada,
    m_qkv,
    v_qkv,
    m_attn,
    v_attn,
    m_in,
    v_in,
    m_out,
    v_out,
):
    seqs, group, width = tokens_in.shape
    heads = width // HD
    factor = HD ** (-0.5)
    flat_rows = seqs * group
    full_ada, full_qkv, full_attn, full_in, full_out = (
        lax.all_gather(w_ada.astype(jnp.bfloat16), ("dp", "seq"), axis=1, tiled=True),
        lax.all_gather(w_qkv.astype(jnp.bfloat16), ("dp", "seq"), axis=0, tiled=True),
        lax.all_gather(w_attn.astype(jnp.bfloat16), ("dp", "seq"), axis=0, tiled=True),
        lax.all_gather(w_in.astype(jnp.bfloat16), ("dp", "seq"), axis=0, tiled=True),
        lax.all_gather(w_out.astype(jnp.bfloat16), ("dp", "seq"), axis=0, tiled=True),
    )
    positions = lax.axis_index("seq") * group + jnp.arange(group, dtype=jnp.int32)
    masked = (positions[None, :] >= span_start[:, None]) & (
        positions[None, :] < (span_start + span_len)[:, None]
    )
    cond_bf = cond_input(timesteps).astype(jnp.bfloat16)
    modulation = jnp.dot(cond_bf, full_ada, preferred_element_type=jnp.float32) + vectors[
        2:8
    ].reshape(1, 6 * width)
    pieces = [modulation[:, which * width : (which + 1) * width][:, None, :] for which in range(6)]
    shift_one, scale_one, gate_one, shift_two, scale_two, gate_two = pieces
    start_tokens = jnp.where(
        masked[..., None], vectors[8][None, None, :], tokens_in.astype(jnp.float32)
    )
    normed_one, inv_one = normalize(start_tokens)
    ln_one = normed_one * vectors[0]
    hidden_one = (
        (ln_one * (1.0 + scale_one) + shift_one).astype(jnp.bfloat16).reshape(flat_rows, width)
    )
    projected = jnp.dot(hidden_one, full_qkv, preferred_element_type=jnp.float32).reshape(
        seqs, group, 3 * width
    )
    cosines, sines = rotary_tables(positions)
    queries = rotate(projected[..., :width].reshape(seqs, group, heads, HD), cosines, sines).astype(
        jnp.bfloat16
    )
    keys_here = rotate(
        projected[..., width : 2 * width].reshape(seqs, group, heads, HD), cosines, sines
    ).astype(jnp.bfloat16)
    values_here = projected[..., 2 * width :].astype(jnp.bfloat16)
    kv_local = jnp.concatenate([keys_here.reshape(seqs, group, width), values_here], axis=-1)
    initial = (
        jnp.full((seqs, heads, group), -1e30, jnp.float32),
        jnp.zeros((seqs, heads, group), jnp.float32),
        jnp.zeros((seqs, heads, group, HD), jnp.float32),
    )
    running, denom, accum = attend_piece(
        initial, lax.all_gather(kv_local, "seq", axis=1, tiled=True), queries, width, factor
    )
    attn_heads = accum / denom[..., None]
    logsum = running + jnp.log(denom)
    attn_rows = jnp.transpose(attn_heads, (0, 2, 1, 3)).reshape(flat_rows, width)
    attn_bf = attn_rows.astype(jnp.bfloat16)
    branch_one = jnp.dot(attn_bf, full_attn, preferred_element_type=jnp.float32).reshape(
        seqs, group, width
    )
    mid_tokens = start_tokens + gate_one * branch_one
    normed_two, inv_two = normalize(mid_tokens)
    ln_two = normed_two * vectors[1]
    hidden_two = (
        (ln_two * (1.0 + scale_two) + shift_two).astype(jnp.bfloat16).reshape(flat_rows, width)
    )
    pre_act = jnp.dot(hidden_two, full_in, preferred_element_type=jnp.float32)
    activ, gelu_back = jax.vjp(partial(jax.nn.gelu, approximate=True), pre_act)
    activ_bf = activ.astype(jnp.bfloat16)
    branch_two = jnp.dot(activ_bf, full_out, preferred_element_type=jnp.float32).reshape(
        seqs, group, width
    )
    block_out = (mid_tokens + gate_two * branch_two).astype(jnp.bfloat16)
    grad_y = cotangent.astype(jnp.float32)
    grad_gate_two = jnp.sum(grad_y * branch_two, axis=1)
    grad_branch_two = (grad_y * gate_two).astype(jnp.bfloat16).reshape(flat_rows, width)
    grad_w_out = jnp.dot(activ_bf.T, grad_branch_two, preferred_element_type=jnp.float32)
    grad_activ = jnp.dot(grad_branch_two, full_out.T, preferred_element_type=jnp.float32)
    grad_pre = gelu_back(grad_activ)[0].astype(jnp.bfloat16)
    grad_w_in = jnp.dot(hidden_two.T, grad_pre, preferred_element_type=jnp.float32)
    grad_hidden_two = jnp.dot(grad_pre, full_in.T, preferred_element_type=jnp.float32).reshape(
        seqs, group, width
    )
    grad_shift_two, grad_scale_two, grad_gain_two, grad_normed_two = mod_back(
        grad_hidden_two, ln_two, normed_two, scale_two, vectors[1]
    )
    grad_mid = grad_y + norm_back(normed_two, inv_two, grad_normed_two)
    grad_gate_one = jnp.sum(grad_mid * branch_one, axis=1)
    grad_branch_one = (grad_mid * gate_one).astype(jnp.bfloat16).reshape(flat_rows, width)
    grad_w_attn = jnp.dot(attn_bf.T, grad_branch_one, preferred_element_type=jnp.float32)
    grad_attn_bf = (
        jnp.dot(grad_branch_one, full_attn.T, preferred_element_type=jnp.float32)
        .astype(jnp.bfloat16)
        .reshape(seqs, group, heads, HD)
    )
    delta = jnp.einsum("sqhd,shqd->shq", grad_attn_bf.astype(jnp.float32), attn_heads)
    kv_all = lax.all_gather(kv_local, "seq", axis=1, tiled=True)
    grad_queries = query_grads(kv_all, queries, grad_attn_bf, logsum, delta, width, factor)
    grad_kv = jnp.transpose(
        lax.psum_scatter(
            key_grads(
                kv_all,
                queries,
                grad_attn_bf,
                logsum,
                delta,
                width,
                factor,
                group * lax.axis_size("seq"),
            ).astype(jnp.bfloat16),
            "seq",
            scatter_dimension=0,
            tiled=True,
        ).astype(jnp.float32),
        (1, 0, 2),
    )
    grad_keys = grad_kv[..., :width].reshape(seqs, group, heads, HD)
    grad_qkv = jnp.concatenate(
        [
            rotate_back(grad_queries, cosines, sines).reshape(seqs, group, width),
            rotate_back(grad_keys, cosines, sines).reshape(seqs, group, width),
            grad_kv[..., width:],
        ],
        axis=-1,
    )
    grad_qkv = grad_qkv.astype(jnp.bfloat16).reshape(flat_rows, 3 * width)
    grad_w_qkv = jnp.dot(hidden_one.T, grad_qkv, preferred_element_type=jnp.float32)
    grad_hidden_one = jnp.dot(grad_qkv, full_qkv.T, preferred_element_type=jnp.float32).reshape(
        seqs, group, width
    )
    grad_shift_one, grad_scale_one, grad_gain_one, grad_normed_one = mod_back(
        grad_hidden_one, ln_one, normed_one, scale_one, vectors[0]
    )
    grad_start = grad_mid + norm_back(normed_one, inv_one, grad_normed_one)
    grad_mask_row = jnp.sum(jnp.where(masked[..., None], grad_start, 0.0), axis=(0, 1))
    grad_input = jnp.where(masked[..., None], 0.0, grad_start)
    grad_mod = jnp.concatenate(
        [
            grad_shift_one,
            grad_scale_one,
            grad_gate_one,
            grad_shift_two,
            grad_scale_two,
            grad_gate_two,
        ],
        axis=1,
    )
    grad_w_ada = jnp.dot(cond_bf.astype(jnp.float32).T, grad_mod, precision=lax.Precision.HIGHEST)
    grad_vectors = jnp.concatenate(
        [
            grad_gain_one[None, :],
            grad_gain_two[None, :],
            jnp.sum(grad_mod, axis=0).reshape(6, width),
            grad_mask_row[None, :],
        ],
        axis=0,
    )
    red_ada, red_qkv, red_attn, red_in, red_out, red_vec = (
        lax.psum_scatter(grad_w_ada, ("dp", "seq"), scatter_dimension=1, tiled=True),
        lax.psum_scatter(grad_w_qkv, ("dp", "seq"), scatter_dimension=0, tiled=True),
        lax.psum_scatter(grad_w_attn, ("dp", "seq"), scatter_dimension=0, tiled=True),
        lax.psum_scatter(grad_w_in, ("dp", "seq"), scatter_dimension=0, tiled=True),
        lax.psum_scatter(grad_w_out, ("dp", "seq"), scatter_dimension=0, tiled=True),
        lax.psum_scatter(grad_vectors, ("dp", "seq"), scatter_dimension=1, tiled=True),
    )
    local_squares = jnp.float32(0.0)
    for reduced in (red_vec, red_ada, red_qkv, red_attn, red_in, red_out):
        local_squares = local_squares + jnp.sum(reduced * reduced)
    grad_norm = jnp.sqrt(lax.psum(local_squares, ("dp", "seq")))
    clip_factor = jnp.minimum(1.0, CLIP / (grad_norm + 1e-06))
    columns = red_vec.shape[1]
    own_vectors = lax.dynamic_slice_in_dim(
        vectors, lax.axis_index(("dp", "seq")) * columns, columns, 1
    )
    vec_out = adam_step(own_vectors, red_vec * clip_factor, m_vec, v_vec, RATE_VECTORS, 0.0)
    ada_out = adam_step(w_ada, red_ada * clip_factor, m_ada, v_ada, RATE, DECAY)
    qkv_out = adam_step(w_qkv, red_qkv * clip_factor, m_qkv, v_qkv, RATE, DECAY)
    attn_out = adam_step(w_attn, red_attn * clip_factor, m_attn, v_attn, RATE, DECAY)
    in_out = adam_step(w_in, red_in * clip_factor, m_in, v_in, RATE, DECAY)
    out_out = adam_step(w_out, red_out * clip_factor, m_out, v_out, RATE, DECAY)
    return (
        block_out,
        grad_input,
        grad_norm,
        vec_out[0],
        vec_out[1],
        vec_out[2],
        ada_out[0],
        ada_out[1],
        ada_out[2],
        qkv_out[0],
        qkv_out[1],
        qkv_out[2],
        attn_out[0],
        attn_out[1],
        attn_out[2],
        in_out[0],
        in_out[1],
        in_out[2],
        out_out[0],
        out_out[1],
        out_out[2],
    )


F32, BF = jnp.float32, jnp.bfloat16
MESH = pl.DeviceIdType.MESH
DP, LINE, SEQ, CHIPS, ALL = 4, 4, 8, 16, 32
ROWS, WIDTH, PACK = 128, 768, 640
HALF = WIDTH // 2
HALVES = ((0, 0), (0, 1), (0, 2), (2, 2), (1, 0), (1, 1), (1, 2), None, (2, 0), (2, 1))

def numbered(**counts):
    at = {}
    for name, count in counts.items():
        at[name] = sum(counts[other] for other in at)
    return SimpleNamespace(**at), sum(counts.values())


S, SEM_COUNT = numbered(
    cond=1,
    mix_qkv=1,
    mix_in=1,
    mix_attn=1,
    mod=1,
    w_qkv=1,
    w_attn=1,
    w_in=1,
    w_out=1,
    group_qkv=1,
    group_attn=1,
    fw_qkv=1,
    fw_attn=1,
    fw_in=1,
    fw_out=1,
    tok=4,
    h2=4,
    dm=4,
    xf=4,
    o=1,
    mm=1,
    dh2=1,
    do=1,
    gp=1,
    dh1=1,
    pair_out=1,
    pair_in=1,
    pair_attn=1,
    pair_qkv=1,
    plane_attn=1,
    plane_qkv=1,
    line_out=1,
    line_in=1,
    line_attn=1,
    line_qkv=1,
    last_in=1,
    last_attn=1,
    last_qkv=1,
    early=1,
    early2=1,
    late=1,
    late2=1,
    sq=1,
)

SCRATCH = dict(
    wide_qkv=((48, 3072), F32),
    wide_in=((48, 3072), F32),
    wide_attn=((48, 768), F32),
    s_qkv=((48, 3072), BF),
    s_in=((48, 3072), BF),
    s_attn=((48, 768), BF),
    s_out=((96, 768), BF),
    w_qkv=((768, 768), BF),
    w_in=((768, 768), BF),
    w_attn=((768, 768), BF),
    w_out=((4, 2, 96, 768), BF),
    conds_all=((4, 8, 128), F32),
    mod_send=((4, 4, 128), F32),
    mod_got=((32, 4, 128), F32),
    mod_flat=((40, 128), F32),
    mod_pad=((8, 384), F32),
    turn=((2, 4, 128, 128), F32),
    dmod_flat=((4, 40, 128), F32),
    mod=((8, 768), F32),
    x0=((128, 768), F32),
    n1=((128, 768), F32),
    inv1=((128, 128), F32),
    x1=((128, 768), F32),
    n2=((128, 768), F32),
    inv2=((128, 128), F32),
    a=((128, 768), F32),
    dx1=((128, 768), F32),
    toks=((4, 128, 768), BF),
    h1=((4, 128, 768), BF),
    h2=((4, 128, 768), BF),
    dm=((4, 128, 768), BF),
    gb=((4, 128, 768), BF),
    du=((4, 128, 768), BF),
    xb=((2, 4, 128, 640), BF),
    pt=((3, 1024, 512), BF),
    ot=((2, 128, 512), F32),
    os=((4, 128, 256), BF),
    ob=((4, 128, 256), BF),
    mms=((4, 128, 768), BF),
    mmr=((4, 128, 768), BF),
    dhs=((4, 128, 768), BF),
    dhr=((4, 128, 768), BF),
    das=((128, 768), BF),
    dos=((4, 128, 256), BF),
    dob=((4, 128, 256), BF),
    dst=((3, 1024, 512), BF),
    ga=((512, 640), F32),
    gps=((512, 512), BF),
    gpr=((512, 512), BF),
    dqkv=((4, 128, 768), BF),
    d1s=((4, 128, 768), BF),
    d1r=((4, 128, 768), BF),
    g_out=((4, 2, 96, 768), BF),
    g_in=((2, 768, 384), BF),
    g_attn=((2, 768, 384), BF),
    g_qkv=((2, 768, 384), BF),
    p_out=((4, 96, 768), BF),
    p_in=((768, 384), BF),
    p_attn=((768, 384), BF),
    p_qkv=((768, 384), BF),
    q_attn=((4, 192, 384), BF),
    q_qkv=((4, 192, 384), BF),
    m_attn=((192, 384), BF),
    m_qkv=((192, 384), BF),
    r_out=((4, 96, 768), BF),
    r_in=((16, 48, 384), BF),
    r_attn=((4, 48, 384), BF),
    r_qkv=((4, 48, 384), BF),
    t_in=((4, 48, 384), F32),
    t_attn=((1, 48, 384), F32),
    t_qkv=((4, 48, 384), F32),
    f_in=((4, 2, 24, 384), F32),
    f_attn=((1, 2, 24, 384), F32),
    f_qkv=((4, 2, 24, 384), F32),
    early=((8, 768), F32),
    early_got=((8, 8, 768), F32),
    early_all=((4, 8, 768), F32),
    late=((4, 768), F32),
    late_got=((8, 4, 768), F32),
    late_all=((4, 4, 768), F32),
    sq=((32, 1, 128), F32),
)


def dot(left, right):
    return jnp.dot(left, right, preferred_element_type=F32)


def dot_nt(left, right):
    return lax.dot_general(left, right, (((1,), (1,)), ((), ())), preferred_element_type=F32)


def dot_tn(left, right):
    return lax.dot_general(left, right, (((0,), (0,)), ((), ())), preferred_element_type=F32)


def loop(count, body, start=0):
    def step(index, carry):
        body(index)
        return carry

    lax.fori_loop(start, count, step, 0)


def layer_kernel(
    i_time,
    i_start,
    i_len,
    i_tok,
    i_cot,
    i_vec,
    i_wada,
    i_wqkv,
    i_wattn,
    i_win,
    i_wout,
    o_y,
    o_dx,
    o_norm,
    o_gqkv,
    o_gattn,
    o_gin,
    o_gout,
    o_dmod,
    o_gvec,
    o_vec,
    o_conds,
    *scratch,
):
    r = SimpleNamespace(**dict(zip(SCRATCH, scratch)))
    send_sems, recv_sems = scratch[-2:]
    b, s = lax.axis_index("dp"), lax.axis_index("seq")
    z, c = lax.div(s, 2), lax.rem(s, 2)
    mate = s + 1 - 2 * c
    chip = b * LINE + z
    me = b * SEQ + s
    drains = []

    def push(src, dst, at, to_b, to_s):
        pltpu.make_async_remote_copy(
            src_ref=src,
            dst_ref=dst,
            send_sem=send_sems.at[at],
            recv_sem=recv_sems.at[at],
            device_id=(to_b, to_s),
            device_id_type=MESH,
        ).start()

    def keep(src, dst, at):
        pltpu.make_async_copy(src, dst, recv_sems.at[at]).start()

    def got(at, like):
        pltpu.make_async_copy(like, like, recv_sems.at[at]).wait()

    def left(at, like):
        pltpu.make_async_copy(like, like, send_sems.at[at]).wait()

    def sent(at, like):
        drains.append((at, like))

    near = (b, b + 1 - 2 * lax.rem(b, 2), b + 2 - 4 * lax.div(b, 2), 3 - b)

    def peers(body):
        for k in (1, 2, 3):
            body(k, near[k])

    def stack(body):
        for k in (1, 2, 3):
            body(lax.rem(z + k, LINE))

    lane = lax.broadcasted_iota(jnp.int32, (1, 128), 1)
    low = lane < 64
    own24 = pl.ds(pl.multiple_of(24 * c, 8), 24)
    mate24 = pl.ds(pl.multiple_of(24 * (1 - c), 8), 24)
    part = pl.ds(pl.multiple_of(HALF * c, 128), HALF)
    chip_rows = pl.ds(pl.multiple_of(48 * chip, 16), 48)
    group_rows = pl.ds(pl.multiple_of(192 * b, 16), 192)

    barrier = pltpu.get_barrier_semaphore()

    def greet(k):
        other = lax.rem(me + k, ALL)
        pl.semaphore_signal(
            barrier, inc=1, device_id=(lax.div(other, SEQ), lax.rem(other, SEQ)), device_id_type=MESH
        )

    loop(ALL, greet, 1)

    def natural(kind, p, head):
        return kind * WIDTH + 192 * p + 64 * head

    def half_at(ref, column, high):
        tile = ref[:, column // 128 * 128 : column // 128 * 128 + 128]
        return tile if (column % 128 == 64) == high else pltpu.roll(tile, 64, 1)

    for p in range(4):
        for tile in range(5):
            pair = []
            for high in (0, 1):
                which = HALVES[2 * tile + high]
                pair.append(
                    jnp.zeros((24, 128), F32)
                    if which is None
                    else half_at(i_wqkv, natural(which[0], p, which[1]), bool(high))
                )
            r.wide_qkv[own24, 768 * p + 128 * tile : 768 * p + 128 * tile + 128] = jnp.where(
                low, pair[0], pair[1]
            )
        r.wide_qkv[own24, 768 * p + 640 : 768 * p + 768] = jnp.zeros((24, 128), F32)
    r.wide_in[own24, :] = i_win[...]
    r.wide_attn[own24, :] = i_wattn[...]
    r.s_out[...] = i_wout[...].astype(BF)
    lanes8 = lax.broadcasted_iota(jnp.int32, (8, 128), 1)
    half_cond = COND // 2
    speed = jnp.exp((lanes8 % half_cond).astype(F32) * (-math.log(10000.0) / half_cond))
    angle = i_time[0].astype(F32) * speed
    wave = jnp.where(lanes8 < half_cond, jnp.cos(angle), jnp.sin(angle))
    r.conds_all[b] = wave * (1.0 / (1.0 + jnp.exp(-wave)))
    pl.semaphore_wait(barrier, ALL - 1)

    def stack_rows(to):
        push(r.s_out, r.w_out.at[z, c], S.w_out, b, 2 * to + c)

    peers(lambda k, to: push(r.conds_all.at[b], r.conds_all.at[b], S.cond, to, s))
    sent(S.cond, r.conds_all.at[0:3])
    stack(lambda to: push(i_tok.at[0], r.toks.at[z], S.tok + z, b, 2 * to + c))
    sent(S.tok + z, r.toks.at[0:3])
    push(r.wide_qkv.at[own24], r.wide_qkv.at[own24], S.mix_qkv, b, mate)
    sent(S.mix_qkv, r.wide_qkv.at[0:24])
    push(r.wide_attn.at[own24], r.wide_attn.at[own24], S.mix_attn, b, mate)
    sent(S.mix_attn, r.wide_attn.at[0:24])
    push(r.wide_in.at[own24], r.wide_in.at[own24], S.mix_in, b, mate)
    sent(S.mix_in, r.wide_in.at[0:24])

    got(S.cond, r.conds_all.at[0:3])
    row8 = lax.broadcasted_iota(jnp.int32, (8, 128), 0)
    cond4 = jnp.zeros((8, 128), F32)
    for k in range(4):
        cond4 = jnp.where(row8 == k, r.conds_all[k], cond4)
    o_conds[...] = cond4
    wide = i_wada.shape[0]
    r.mod_pad[...] = jnp.zeros((8, 384), F32)
    r.mod_pad[:, 0:wide] = dot_nt(cond4.astype(BF), i_wada[...].astype(BF))
    columns = pltpu.roll(r.mod_pad[...], lax.rem(wide * me, 128), 1)
    for k in range(4):
        for t in range(3):
            r.mod_send[k, t : t + 1, :] = columns[k : k + 1, 128 * t : 128 * t + 128]
        r.mod_send[k, 3:4, :] = jnp.zeros((1, 128), F32)

    def send_mod(k):
        other = lax.rem(me + k, ALL)
        ob = lax.div(other, SEQ)
        push(r.mod_send.at[ob], r.mod_got.at[me], S.mod, ob, lax.rem(other, SEQ))

    loop(ALL, send_mod, 1)
    sent(S.mod, r.mod_got.at[0:31])
    keep(r.mod_send.at[b], r.mod_got.at[me], S.mod)

    def block(src, first):
        return src.at[:, pl.ds(pl.multiple_of(first, 128), HALF)]

    def spread(src, dst, at):
        def one(k):
            to = lax.rem(chip + k, CHIPS)
            to_b, to_z = lax.div(to, LINE), lax.rem(to, LINE)
            push(
                block(src, WIDTH * to_b + HALF * c),
                dst.at[chip_rows, part],
                at,
                to_b,
                2 * to_z + c,
            )

        loop(CHIPS, one, 1)
        keep(block(src, WIDTH * b + HALF * c), dst.at[chip_rows, part], at)
        sent(at, dst.at[0:720, 0:HALF])

    def along_line(src, dst, at, step):
        stack(
            lambda to: push(
                block(src, step * to + HALF * c), dst.at[chip_rows, part], at, b, 2 * to + c
            )
        )
        keep(block(src, step * z + HALF * c), dst.at[chip_rows, part], at)
        sent(at, dst.at[0:144, 0:HALF])

    def over_plane(dst, first, at):
        got(first, dst.at[0:192, 0:HALF])
        peers(
            lambda k, to: push(dst.at[group_rows, part], dst.at[group_rows, part], at, to, s)
        )
        sent(at, dst.at[0:576, 0:HALF])

    def share(dst, at, onward, rows):
        got(at, dst.at[0:rows, 0:HALF])
        push(dst.at[:, part], dst.at[:, part], onward, b, mate)
        sent(onward, dst.at[:, 0:HALF])

    got(S.mix_qkv, r.wide_qkv.at[0:24])
    r.s_qkv[...] = r.wide_qkv[...].astype(BF)
    along_line(r.s_qkv, r.w_qkv, S.w_qkv, WIDTH)
    got(S.mix_attn, r.wide_attn.at[0:24])
    r.s_attn[...] = r.wide_attn[...].astype(BF)
    along_line(r.s_attn, r.w_attn, S.w_attn, 0)

    def start_tokens(tokens, k):
        place = (2 * k + c) * ROWS + lax.broadcasted_iota(jnp.int32, (ROWS, 1), 0)
        hidden = (place >= i_start[0]) & (place < i_start[0] + i_len[0])
        return jnp.where(hidden, i_vec[8:9, :], tokens.astype(F32)), hidden

    x0, _ = start_tokens(i_tok[0], z)
    r.x0[...] = x0
    n1, inv1 = normalize(x0)
    r.n1[...] = n1
    r.inv1[...] = jnp.broadcast_to(inv1, (ROWS, 128))

    got(S.mod, r.mod_got)
    r.mod_flat[...] = jnp.zeros((40, 128), F32)
    for k in range(ALL):
        first = 9 * k // 8
        r.mod_flat[first : first + 3, :] += r.mod_got[k, 0:3, :]
    for k in range(6):
        row = jnp.concatenate(
            [r.mod_flat[6 * k + t : 6 * k + t + 1, :] for t in range(6)], axis=1
        )
        r.mod[k : k + 1, :] = row + i_vec[2 + k : 3 + k, :]

    def mod(k):
        return r.mod[k : k + 1, :]

    def vec(k):
        return i_vec[k : k + 1, :]

    r.h1[z] = (r.n1[...] * vec(0) * (1.0 + mod(1)) + mod(0)).astype(BF)
    r.dm[0] = (i_cot[0].astype(F32) * mod(5)).astype(BF)
    over_plane(r.w_qkv, S.w_qkv, S.group_qkv)
    peers(lambda k, to: push(r.dm.at[0], r.dm.at[k], S.dm + k, to, s))
    for k in (1, 2, 3):
        sent(S.dm + k, r.dm.at[0])

    lanes = lax.broadcasted_iota(jnp.int32, (ROWS, 128), 1)
    first_half = lanes % HD < HD // 2
    speed = jnp.exp((lanes % (HD // 2)).astype(F32) * (-math.log(10000.0) / (HD // 2)))
    row = lax.broadcasted_iota(jnp.int32, (ROWS, 128), 0)

    def table(k):
        angle = ((2 * k + c) * ROWS + row).astype(F32) * speed
        r.turn[0, k] = jnp.cos(angle)
        sine = jnp.sin(angle)
        r.turn[1, k] = jnp.where(first_half, -sine, sine)

    loop(LINE, table)

    got(S.mix_in, r.wide_in.at[0:24])
    r.s_in[...] = r.wide_in[...].astype(BF)

    share(r.w_qkv, S.group_qkv, S.fw_qkv, 576)
    over_plane(r.w_attn, S.w_attn, S.group_attn)
    got(S.fw_qkv, r.w_qkv.at[:, 0:HALF])

    def turned(tile, sign, k):
        other = jnp.where(first_half, pltpu.roll(tile, 96, 1), pltpu.roll(tile, 32, 1))
        return tile * r.turn[0, k] + sign * (other * r.turn[1, k])

    def project(j):
        k = lax.rem(z + j, LINE)

        @pl.when(j > 0)
        def _():
            got(S.tok + k, r.toks.at[0])
            other, _ = start_tokens(r.toks[k], k)
            other, _ = normalize(other)
            r.h1[k] = (other * vec(0) * (1.0 + mod(1)) + mod(0)).astype(BF)

        x = dot(r.h1[k], r.w_qkv[:, 0:PACK])
        tiles = [x[:, 128 * t : 128 * t + 128] for t in range(5)]
        tiles[0] = turned(tiles[0], 1.0, k) * 0.125
        tiles[1] = jnp.where(low, turned(tiles[1], 1.0, k) * 0.125, tiles[1])
        tiles[2] = turned(tiles[2], 1.0, k)
        tiles[3] = turned(tiles[3], 1.0, k)
        for t in range(5):
            r.xb[0, k, :, 128 * t : 128 * t + 128] = tiles[t].astype(BF)
        push(r.xb.at[0, k], r.xb.at[1, k], S.xf + k, b, mate)

    loop(4, project)
    for k in range(4):
        sent(S.xf + k, r.xb.at[0, 0])

    stack(stack_rows)
    keep(r.s_out, r.w_out.at[z, c], S.w_out)
    sent(S.w_out, r.w_out.at[0:3, 0])
    spread(r.s_in, r.w_in, S.w_in)
    for k in range(4):
        got(S.xf + k, r.xb.at[0, 0])

    def tile_of(t):
        return r.xb[:, :, :, 128 * t : 128 * t + 128].reshape(1024, 128)

    heads = ((0, 2, 4, True, True), (0, 2, 4, False, False), (1, 3, 1, True, False))

    def queries(head, first, size):
        q_tile, _, _, q_low, _ = heads[head]
        q = r.xb[0, first : first + size, :, 128 * q_tile : 128 * q_tile + 128]
        return jnp.where(low if q_low else ~low, q.reshape(size * 128, 128), jnp.zeros((), BF))

    for half in range(2):
        at = slice(256 * half, 256 * half + 256)
        for head in range(3):
            scores = dot_nt(tile_of(heads[head][1]), queries(head, 2 * half, 2))
            weights = jnp.exp(scores - jnp.max(scores, axis=0, keepdims=True))
            weights = weights * (1.0 / jnp.sum(weights, axis=0, keepdims=True))
            weights = weights.astype(BF)
            r.pt[head, :, at] = weights
            out = dot_tn(tile_of(heads[head][2]), weights)
            if head == 0:
                r.ot[0, 0:64, at] = out[0:64]
            elif head == 1:
                r.ot[0, 64:128, at] = out[64:128]
            else:
                r.ot[1, 0:64, at] = out[64:128]
                r.ot[1, 64:128, at] = jnp.zeros((64, 256), F32)
        for t in range(2):
            r.os[2 * half : 2 * half + 2, :, 128 * t : 128 * t + 128] = (
                r.ot[t, :, at].T.astype(BF).reshape(2, 128, 128)
            )
        for to in (2 * half, 2 * half + 1):

            @pl.when(z == to)
            def _():
                keep(r.os.at[to], r.ob.at[z], S.o)

            @pl.when(z != to)
            def _():
                push(r.os.at[to], r.ob.at[z], S.o, b, 2 * to + c)

    sent(S.o, r.os.at[0:3])
    share(r.w_attn, S.group_attn, S.fw_attn, 576)
    got(S.fw_attn, r.w_attn.at[:, 0:HALF])
    got(S.o, r.ob)
    a = jnp.zeros((ROWS, WIDTH), F32)
    for p in range(4):
        a += dot(r.ob[p, :, 0:128], r.w_attn[192 * p : 192 * p + 128, :])
        a += dot(r.ob[p, :, 128:192], r.w_attn[192 * p + 128 : 192 * p + 192, :])
    r.a[...] = a
    x1 = r.x0[...] + mod(2) * a
    r.x1[...] = x1
    n2, inv2 = normalize(x1)
    r.n2[...] = n2
    r.inv2[...] = jnp.broadcast_to(inv2, (ROWS, 128))
    r.h2[0] = (n2 * vec(1) * (1.0 + mod(4)) + mod(3)).astype(BF)
    peers(lambda k, to: push(r.h2.at[0], r.h2.at[k], S.h2 + k, to, s))
    for k in (1, 2, 3):
        sent(S.h2 + k, r.h2.at[0])
    got(S.w_out, r.w_out.at[:, 0])
    push(r.w_out.at[:, c], r.w_out.at[:, c], S.fw_out, b, mate)
    sent(S.fw_out, r.w_out.at[:, 0])
    share(r.w_in, S.w_in, S.fw_in, 768)
    got(S.fw_out, r.w_out.at[:, 0])
    got(S.fw_in, r.w_in.at[:, 0:HALF])

    def feed(first, count):
        at = slice(first, first + count)
        size = count * ROWS
        u = dot(r.h2[at].reshape(size, WIDTH), r.w_in[...])
        slope = 0.7978845608028654
        cube = 0.044715
        t = jnp.tanh(slope * (u + cube * u * u * u))
        r.gb[at] = (0.5 * u * (1.0 + t)).astype(BF).reshape(count, ROWS, WIDTH)
        bend = 0.5 * (1.0 + t) + 0.5 * u * (1.0 - t * t) * (slope * (1.0 + 3.0 * cube * u * u))
        back = dot_nt(r.dm[at].reshape(size, WIDTH), r.w_out[...].reshape(WIDTH, WIDTH))
        du = (back * bend).astype(BF)
        r.du[at] = du.reshape(count, ROWS, WIDTH)
        r.dhs[at] = dot_nt(du, r.w_in[...]).astype(BF).reshape(count, ROWS, WIDTH)

    feed(0, 1)
    for first, count in ((1, 2), (3, 1)):
        for k in range(first, first + count):
            got(S.h2 + k, r.h2.at[0])
            got(S.dm + k, r.dm.at[0])
        feed(first, count)
        for k in range(first, first + count):
            push(r.dhs.at[k], r.dhr.at[k], S.dh2, near[k], s)
    sent(S.dh2, r.dhs.at[0:3])
    for t in range(3):
        at = slice(256 * t, 256 * t + 256)
        mm = dot(r.gb[...].reshape(512, WIDTH), r.w_out[:, :, :, at].reshape(WIDTH, 256))
        r.mms[:, :, at] = mm.astype(BF).reshape(4, ROWS, 256)
    peers(lambda k, to: push(r.mms.at[k], r.mmr.at[k], S.mm, to, s))
    sent(S.mm, r.mms.at[0:3])

    def gather(own, others):
        total = own[0].astype(F32)
        for k in (1, 2, 3):
            total += others[k].astype(F32)
        return total

    for k in range(2):
        rows = slice(384 * k, 384 * k + 384)
        result = dot_tn(r.gb[:, :, rows].reshape(512, 384), r.dm[...].reshape(512, 768))
        r.g_out[2 * k : 2 * k + 2] = result.astype(BF).reshape(2, 2, 96, 768)
    push(r.g_out.at[:, 1 - c], r.p_out, S.pair_out, b, mate)
    sent(S.pair_out, r.p_out)

    def outer(left, right, dst):
        for k in range(2):
            rows = slice(384 * k, 384 * k + 384)
            result = dot_tn(
                left[:, :, rows].reshape(512, 384), right[...].reshape(512, 768)
            ).astype(BF)
            dst[0, rows, :] = result[:, 0:HALF]
            dst[1, rows, :] = result[:, HALF:WIDTH]

    def to_mate(grad, dst, at):
        push(grad.at[1 - c], dst, at, b, mate)
        sent(at, dst)

    def pair_sum(grad, pair, at):
        got(at, pair)
        grad[c] = (grad[c].astype(F32) + pair[...].astype(F32)).astype(BF)

    def plane_sum(grad, dst, at):
        def rows(to):
            return grad.at[c, pl.ds(pl.multiple_of(192 * to, 16), 192)]

        peers(lambda k, to: push(rows(to), dst.at[k], at, to, s))
        keep(rows(b), dst.at[0], at)
        sent(at, dst.at[0:3])

    def line_sum(src, total, dst, first, at):
        got(first, src)
        total[...] = (
            (src[0].astype(F32) + src[1].astype(F32)) + (src[2].astype(F32) + src[3].astype(F32))
        ).astype(BF)

        def rows(to):
            return total.at[pl.ds(pl.multiple_of(48 * to, 16), 48)]

        stack(lambda to: push(rows(to), dst.at[z], at, b, 2 * to + c))
        keep(rows(z), dst.at[z], at)
        sent(at, dst.at[0:3])

    def trade(total, final, at):
        push(total.at[:, mate24], final.at[:, c], at, b, mate)
        sent(at, final.at[:, 0])
        final[:, c] = total[:, own24, :]

    outer(r.h2, r.du, r.g_in)
    to_mate(r.g_in, r.p_in, S.pair_in)

    got(S.pair_out, r.p_out)
    for k in range(4):
        r.g_out[k, c] = (r.g_out[k, c].astype(F32) + r.p_out[k].astype(F32)).astype(BF)

    def send_gout(to):
        push(r.g_out.at[to, c], r.r_out.at[z], S.line_out, b, 2 * to + c)

    stack(send_gout)
    keep(r.g_out.at[z, c], r.r_out.at[z], S.line_out)
    sent(S.line_out, r.r_out.at[0:3])

    got(S.dh2, r.dhr.at[0:3])
    dh = gather(r.dhs, r.dhr)
    n2 = r.n2[...]
    inv2 = r.inv2[:, 0:1]
    r.early[...] = jnp.zeros((8, 768), F32)
    r.early[2:3, :] = jnp.sum(dh, axis=0, keepdims=True)
    both = jnp.sum(dh * n2, axis=0, keepdims=True)
    r.early[3:4, :] = both * vec(1)
    r.early[0:1, :] = both * (1.0 + mod(4))
    grad = dh * ((1.0 + mod(4)) * vec(1))
    dx1 = i_cot[0].astype(F32) + norm_back(n2, inv2, grad)
    r.dx1[...] = dx1
    r.early[1:2, :] = jnp.sum(dx1 * r.a[...], axis=0, keepdims=True)
    r.das[...] = (dx1 * mod(2)).astype(BF)
    for p in range(4):
        first = 192 * p
        r.dos[p, :, 0:128] = dot_nt(r.das[...], r.w_attn[first : first + 128, :]).astype(BF)
        tail = dot_nt(r.das[...], r.w_attn[first + 128 : first + 192, :])
        r.dos[p, :, 128:256] = jnp.concatenate(
            [tail, jnp.zeros((ROWS, 64), F32)], axis=1
        ).astype(BF)

    stack(lambda to: push(r.dos.at[to], r.dob.at[z], S.do, b, 2 * to + c))
    keep(r.dos.at[z], r.dob.at[z], S.do)
    sent(S.do, r.dos.at[0:3])

    for p in range(4):
        rows = slice(192 * p, 192 * p + 192)
        result = dot_tn(r.ob[p], r.das[...])[0:192].astype(BF)
        r.g_attn[0, rows, :] = result[:, 0:HALF]
        r.g_attn[1, rows, :] = result[:, HALF:WIDTH]
    to_mate(r.g_attn, r.p_attn, S.pair_attn)

    got(S.mm, r.mmr.at[0:3])
    mm = gather(r.mms, r.mmr)
    o_y[...] = (r.x1[...] + mod(5) * mm).astype(BF)
    r.early[4:5, :] = jnp.sum(i_cot[0].astype(F32) * mm, axis=0, keepdims=True)

    def over_line(src, dst, name):
        def one(k):
            push(src, dst.at[s], name, b, lax.rem(s + k, SEQ))

        loop(SEQ, one, 1)
        keep(src, dst.at[s], name)
        sent(name, dst.at[0:7])

    def over_group(got_ref, dst, name):
        total = got_ref[0]
        for k in range(1, SEQ):
            total += got_ref[k]
        dst[b] = total
        peers(lambda k, to: push(dst.at[b], dst.at[b], name, to, s))
        sent(name, dst.at[0:3])

    over_line(r.early, r.early_got, S.early)

    pair_sum(r.g_in, r.p_in, S.pair_in)

    def send_gin(k):
        to = lax.rem(chip + k, CHIPS)
        push(
            r.g_in.at[c, pl.ds(pl.multiple_of(48 * to, 16), 48)],
            r.r_in.at[chip],
            S.line_in,
            lax.div(to, LINE),
            2 * lax.rem(to, LINE) + c,
        )

    loop(CHIPS, send_gin, 1)
    keep(r.g_in.at[c, chip_rows], r.r_in.at[chip], S.line_in)
    sent(S.line_in, r.r_in.at[0:15])
    pair_sum(r.g_attn, r.p_attn, S.pair_attn)
    plane_sum(r.g_attn, r.q_attn, S.plane_attn)

    got(S.do, r.dob)
    dot0, dot1 = r.dob[:, :, 0:128].reshape(512, 128), r.dob[:, :, 128:256].reshape(512, 128)
    zero = jnp.zeros((), BF)
    moved = pltpu.roll(dot1.astype(F32), 64, 1).astype(BF)
    grads = (jnp.where(low, dot0, zero), jnp.where(low, zero, dot0), moved)
    product = dot0.astype(F32).T * r.ot[0]
    deltas = (
        jnp.sum(product[0:64], axis=0, keepdims=True),
        jnp.sum(product[64:128], axis=0, keepdims=True),
        jnp.sum(dot1.astype(F32).T * r.ot[1], axis=0, keepdims=True),
    )
    for head in range(3):
        values = tile_of(heads[head][2])
        for half in range(2):
            at = slice(256 * half, 256 * half + 256)
            dp = dot_nt(values, grads[head][at])
            r.dst[head, :, at] = (
                r.pt[head, :, at].astype(F32) * (dp - deltas[head][:, at])
            ).astype(BF)

    def key_grads(rows):
        dk = [dot(r.dst[head, rows, :], queries(head, 0, 4)) for head in range(3)]
        dv = [dot(r.pt[head, rows, :], grads[head]) for head in range(3)]
        return (dv[2], dk[0] + dk[1], dk[2], dv[0] + dv[1])

    for t, tile in enumerate(key_grads(slice(512, 1024))):
        r.gps[:, 128 * t : 128 * t + 128] = tile.astype(BF)
    push(r.gps, r.gpr, S.gp, b, mate)
    sent(S.gp, r.gps)
    for t, tile in enumerate(key_grads(slice(0, 512))):
        r.ga[:, 128 * t + 128 : 128 * t + 256] = tile
    for half in range(2):
        at = slice(256 * half, 256 * half + 256)
        turned_q = [dot_tn(tile_of(heads[head][1]), r.dst[head, :, at]) for head in range(3)]
        top = jnp.concatenate([turned_q[0][0:64], turned_q[1][64:128]], axis=0)
        r.ga[at, 0:128] = top.T * 0.125
        r.ga[at, 128:256] += turned_q[2].T * 0.125
    got(S.gp, r.gpr)

    def unproject(j):
        k = lax.rem(z + 1 + j, LINE)
        rows = pl.ds(pl.multiple_of(128 * k, 128), 128)
        tiles = [r.ga[rows, 0:128]] + [
            r.ga[rows, 128 * t : 128 * t + 128]
            + r.gpr[rows, 128 * t - 128 : 128 * t].astype(F32)
            for t in range(1, 5)
        ]
        tiles[0] = turned(tiles[0], -1.0, k)
        tiles[1] = jnp.where(low, turned(tiles[1], -1.0, k), tiles[1])
        tiles[2] = turned(tiles[2], -1.0, k)
        tiles[3] = turned(tiles[3], -1.0, k)
        for t in range(5):
            r.dqkv[k, :, 128 * t : 128 * t + 128] = tiles[t].astype(BF)
        r.dqkv[k, :, PACK:WIDTH] = jnp.zeros((128, 128), BF)
        r.d1s[k] = dot_nt(r.dqkv[k, :, 0:PACK], r.w_qkv[:, 0:PACK]).astype(BF)

        @pl.when(j < 3)
        def _():
            push(r.d1s.at[k], r.d1r.at[z], S.dh1, b, 2 * k + c)

    loop(4, unproject)
    sent(S.dh1, r.d1s.at[0:3])
    outer(r.h1, r.dqkv, r.g_qkv)
    to_mate(r.g_qkv, r.p_qkv, S.pair_qkv)
    line_sum(r.q_attn, r.m_attn, r.r_attn, S.plane_attn, S.line_attn)
    got(S.early, r.early_got)
    over_group(r.early_got, r.early_all, S.early2)
    pair_sum(r.g_qkv, r.p_qkv, S.pair_qkv)
    plane_sum(r.g_qkv, r.q_qkv, S.plane_qkv)

    got(S.line_in, r.r_in)
    for p in range(4):
        r.t_in[p] = (r.r_in[4 * p].astype(F32) + r.r_in[4 * p + 1].astype(F32)) + (
            r.r_in[4 * p + 2].astype(F32) + r.r_in[4 * p + 3].astype(F32)
        )
    trade(r.t_in, r.f_in, S.last_in)
    line_sum(r.q_qkv, r.m_qkv, r.r_qkv, S.plane_qkv, S.line_qkv)

    got(S.dh1, r.d1r.at[0:3])
    dh = r.d1s[z].astype(F32)
    for k in (1, 2, 3):
        dh += r.d1r[lax.rem(z + k, LINE)].astype(F32)
    n1 = r.n1[...]
    both = jnp.sum(dh * n1, axis=0, keepdims=True)
    r.late[0:1, :] = both * (1.0 + mod(1))
    r.late[1:2, :] = jnp.sum(dh, axis=0, keepdims=True)
    r.late[2:3, :] = both * vec(0)
    grad = dh * ((1.0 + mod(1)) * vec(0))
    dx0 = r.dx1[...] + norm_back(n1, r.inv1[:, 0:1], grad)
    _, hidden = start_tokens(i_tok[0], z)
    o_dx[...] = jnp.where(hidden, 0.0, dx0)
    r.late[3:4, :] = jnp.sum(jnp.where(hidden, dx0, 0.0), axis=0, keepdims=True)
    over_line(r.late, r.late_got, S.late)

    got(S.line_out, r.r_out)
    total = (r.r_out[0].astype(F32) + r.r_out[1].astype(F32)) + (
        r.r_out[2].astype(F32) + r.r_out[3].astype(F32)
    )
    o_gout[...] = total
    squares = total * total
    squares = jnp.sum(squares[:, 0:128] + squares[:, 128:256] + squares[:, 256:384]
                      + squares[:, 384:512] + squares[:, 512:640] + squares[:, 640:768],
                      axis=0, keepdims=True)

    def fold(value):
        total = value[:, 0:128] * value[:, 0:128]
        for t in range(1, value.shape[1] // 128):
            total += value[:, 128 * t : 128 * t + 128] * value[:, 128 * t : 128 * t + 128]
        return jnp.sum(total, axis=0, keepdims=True)

    got(S.line_attn, r.r_attn)
    r.t_attn[0] = (r.r_attn[0].astype(F32) + r.r_attn[1].astype(F32)) + (
        r.r_attn[2].astype(F32) + r.r_attn[3].astype(F32)
    )
    trade(r.t_attn, r.f_attn, S.last_attn)
    got(S.line_qkv, r.r_qkv)
    r.t_qkv[...] = r.r_qkv[...].astype(F32)
    trade(r.t_qkv, r.f_qkv, S.last_qkv)
    got(S.late, r.late_got)
    over_group(r.late_got, r.late_all, S.late2)
    got(S.last_in, r.f_in.at[:, 0])
    got(S.last_attn, r.f_attn.at[:, 0])
    for h in range(2):
        for p in range(4):
            value = r.f_in[p, h]
            o_gin[:, 768 * p + 384 * h : 768 * p + 384 * h + 384] = value
            squares += fold(value)
        value = r.f_attn[0, h]
        o_gattn[:, 384 * h : 384 * h + 384] = value
        squares += fold(value)
    got(S.last_qkv, r.f_qkv.at[:, 0])
    where = {which: index for index, which in enumerate(HALVES) if which is not None}

    def packed_half(chunk, high):
        kind, rest = chunk // 12, chunk % 12
        index = where[(kind, rest % 3)]
        t = index // 2
        tile = r.f_qkv[rest // 3, t // 3, :, t % 3 * 128 : t % 3 * 128 + 128]
        return tile if index % 2 == high else pltpu.roll(tile, 64, 1)

    for t in range(18):
        o_gqkv[:, 128 * t : 128 * t + 128] = jnp.where(
            low, packed_half(2 * t, 0), packed_half(2 * t + 1, 1)
        )
    for p in range(4):
        for h in range(2):
            squares += fold(r.f_qkv[p, h])

    r.sq[me] = squares

    def send_sq(k):
        other = lax.rem(me + k, ALL)
        push(r.sq.at[me], r.sq.at[me], S.sq, lax.div(other, SEQ), lax.rem(other, SEQ))

    loop(ALL, send_sq, 1)
    sent(S.sq, r.sq.at[0:31])
    got(S.early2, r.early_all.at[0:3])
    got(S.late2, r.late_all.at[0:3])
    mods = []
    for k in range(4):
        early, late = r.early_all[k], r.late_all[k]
        rows = jnp.concatenate([late[1:3], early[1:5], jnp.zeros((2, 768), F32)], axis=0)
        for n in range(6):
            for m in range(6):
                r.dmod_flat[k, 6 * n + m : 6 * n + m + 1, :] = rows[
                    n : n + 1, 128 * m : 128 * m + 128
                ]
        mods.append(rows)
    gain = jnp.concatenate(
        [
            sum(r.late_all[k][0:1] for k in range(4)),
            sum(r.early_all[k][0:1] for k in range(4)),
            (mods[0] + mods[1] + mods[2] + mods[3])[0:6],
        ],
        axis=0,
    )
    mask_row = sum(r.late_all[k][3:4] for k in range(4))
    gains = jnp.concatenate([gain, mask_row, jnp.zeros((7, 768), F32)], axis=0)
    masters = jnp.concatenate([i_vec[...], jnp.zeros((7, 768), F32)], axis=0)
    own = lax.rem(WIDTH - 24 * me, WIDTH)
    o_gvec[...] = pltpu.roll(gains, own, 1)[:, 0:128]
    o_vec[...] = pltpu.roll(masters, own, 1)[:, 0:128]
    r.mod_pad[...] = jnp.zeros((8, 384), F32)
    window = lax.div(wide * me, 128)
    for k in range(4):
        rows = r.dmod_flat[k, pl.ds(window, 3), :]
        for m in range(3):
            r.mod_pad[k : k + 1, 128 * m : 128 * m + 128] = rows[m : m + 1, :]
    o_dmod[...] = pltpu.roll(r.mod_pad[...], lax.rem(384 - lax.rem(wide * me, 128), 384), 1)[:, 0:256]
    small = jnp.sum(gain * gain) + jnp.sum(mask_row * mask_row)
    conds = [r.conds_all[k][0:1].astype(BF).astype(F32) for k in range(4)]
    for k in range(4):
        for m in range(k, 4):
            term = jnp.sum(mods[k] * mods[m]) * jnp.sum(conds[k] * conds[m])
            small += term if m == k else 2.0 * term
    got(S.sq, r.sq.at[0:31])
    total = r.sq[0]
    for k in range(1, ALL):
        total += r.sq[k]
    o_norm[...] = jnp.broadcast_to(jnp.sqrt(jnp.sum(total) + small), (8, 128))

    for at, like in drains:
        left(at, like)


def run_layer(*args):
    shapes = (
        ((ROWS, WIDTH), BF),
        ((ROWS, WIDTH), F32),
        ((8, 128), F32),
        ((24, 3 * WIDTH), F32),
        ((24, WIDTH), F32),
        ((24, 4 * WIDTH), F32),
        ((96, WIDTH), F32),
        ((8, 256), F32),
        ((16, 128), F32),
        ((16, 128), F32),
        ((8, 128), F32),
    )
    whole = pl.BlockSpec(memory_space=pltpu.VMEM)
    scalar = pl.BlockSpec(memory_space=pltpu.SMEM)
    return pl.pallas_call(
        layer_kernel,
        out_shape=[jax.ShapeDtypeStruct(shape, kind) for shape, kind in shapes],
        in_specs=[scalar] * 3 + [whole] * (len(args) - 3),
        out_specs=[whole] * len(shapes),
        scratch_shapes=[pltpu.VMEM(shape, kind) for shape, kind in SCRATCH.values()]
        + [pltpu.SemaphoreType.DMA((SEM_COUNT,)), pltpu.SemaphoreType.DMA((SEM_COUNT,))],
        compiler_params=pltpu.CompilerParams(
            collective_id=0, has_side_effects=True, vmem_limit_bytes=60 * 1024 * 1024
        ),
    )(*args)


def finish_kernel(
    y, dx, norm, g_qkv, g_attn, g_in, g_out, dmod, g_vec, own_vec, conds, *rest
):
    (w_ada, w_qkv, w_attn, w_in, w_out), moments, outs = rest[:5], rest[5:17], rest[17:]
    outs[0][0] = y[...]
    outs[1][0] = dx[...]
    outs[2][0, 0] = norm[0, 0]
    clip = jnp.minimum(1.0, CLIP / (norm[0:1, 0:1] + 1e-06))
    columns = w_ada.shape[0]
    rounded = conds[...].astype(BF).astype(F32)
    turned_mod = dmod[...].T
    g_ada = turned_mod[0:columns, 0:1] * rounded[0:1, :]
    for k in range(1, 4):
        g_ada += turned_mod[0:columns, k : k + 1] * rounded[k : k + 1, :]
    narrow = moments[0].shape[1]
    grads = (
        g_vec[0:9, 0:narrow],
        g_ada,
        g_qkv[...],
        g_attn[...],
        g_in[...],
        g_out[...],
    )
    weights = (
        own_vec[0:9, 0:narrow],
        w_ada[...],
        w_qkv[...],
        w_attn[...],
        w_in[...],
        w_out[...],
    )
    for k in range(6):
        results = adam_step(
            weights[k],
            grads[k] * clip,
            moments[2 * k][...],
            moments[2 * k + 1][...],
            RATE if k else RATE_VECTORS,
            DECAY if k else 0.0,
        )
        for n in range(3):
            outs[3 + 3 * k + n][...] = results[n]


def run_finish(partial_results, weights, moments):
    shapes = [((1, ROWS, WIDTH), BF), ((1, ROWS, WIDTH), F32), ((1, 1), F32)]
    for moment in moments[::2]:
        shapes += [(moment.shape, F32)] * 3
    whole = pl.BlockSpec(memory_space=pltpu.VMEM)
    specs = [whole] * len(shapes)
    specs[2] = pl.BlockSpec(memory_space=pltpu.SMEM)
    args = (*partial_results, *weights, *moments)
    return pl.pallas_call(
        finish_kernel,
        out_shape=[jax.ShapeDtypeStruct(shape, kind) for shape, kind in shapes],
        in_specs=[whole] * len(args),
        out_specs=specs,
        compiler_params=pltpu.CompilerParams(vmem_limit_bytes=60 * 1024 * 1024),
    )(*args)


def slices(
    tokens_in,
    cotangent,
    timesteps,
    span_start,
    span_len,
    vectors,
    w_ada,
    w_qkv,
    w_attn,
    w_in,
    w_out,
    m_vec,
    v_vec,
    m_ada,
    v_ada,
    m_qkv,
    v_qkv,
    m_attn,
    v_attn,
    m_in,
    v_in,
    m_out,
    v_out,
):
    partial_results = run_layer(
        timesteps,
        span_start,
        span_len,
        tokens_in,
        cotangent,
        vectors,
        w_ada.T,
        w_qkv,
        w_attn,
        w_in,
        w_out,
    )
    moments = (
        m_vec,
        v_vec,
        m_ada.T,
        v_ada.T,
        m_qkv,
        v_qkv,
        m_attn,
        v_attn,
        m_in,
        v_in,
        m_out,
        v_out,
    )
    results = run_finish(partial_results, (w_ada.T, w_qkv, w_attn, w_in, w_out), moments)
    ada_results = [result.T for result in results[6:9]]
    return (*results[:2], results[2].reshape(()), *results[3:6], *ada_results, *results[9:])


def solution(mesh):
    in_specs = (
        P("dp", "seq", None),
        P("dp", "seq", None),
        P("dp"),
        P("dp"),
        P("dp"),
        P(),
        P(None, ("dp", "seq")),
        P(("dp", "seq"), None),
        P(("dp", "seq"), None),
        P(("dp", "seq"), None),
        P(("dp", "seq"), None),
        P(None, ("dp", "seq")),
        P(None, ("dp", "seq")),
        P(None, ("dp", "seq")),
        P(None, ("dp", "seq")),
        P(("dp", "seq"), None),
        P(("dp", "seq"), None),
        P(("dp", "seq"), None),
        P(("dp", "seq"), None),
        P(("dp", "seq"), None),
        P(("dp", "seq"), None),
        P(("dp", "seq"), None),
        P(("dp", "seq"), None),
    )
    out_specs = (
        P("dp", "seq", None),
        P("dp", "seq", None),
        P(),
        P(None, ("dp", "seq")),
        P(None, ("dp", "seq")),
        P(None, ("dp", "seq")),
        P(None, ("dp", "seq")),
        P(None, ("dp", "seq")),
        P(None, ("dp", "seq")),
        P(("dp", "seq"), None),
        P(("dp", "seq"), None),
        P(("dp", "seq"), None),
        P(("dp", "seq"), None),
        P(("dp", "seq"), None),
        P(("dp", "seq"), None),
        P(("dp", "seq"), None),
        P(("dp", "seq"), None),
        P(("dp", "seq"), None),
        P(("dp", "seq"), None),
        P(("dp", "seq"), None),
        P(("dp", "seq"), None),
    )
    sizes = dict(mesh.shape)
    local = slices if (sizes["dp"], sizes["seq"]) == (4, 8) else plain
    return jax.shard_map(local, mesh=mesh, in_specs=in_specs, out_specs=out_specs, check_vma=False)
```

```python
from functools import partial
import math
from types import SimpleNamespace

import jax
import jax.numpy as jnp
from jax import lax
from jax.experimental import pallas as pl
from jax.experimental.pallas import tpu as pltpu
from jax.sharding import PartitionSpec as P

HD = 64
COND = 128
STEP = 10


BETA_ONE = 0.9
BETA_TWO = 0.999
ADAM_EPS = 1e-08
RATE = 0.1
RATE_VECTORS = 0.3
DECAY = 0.01
CLIP = 1.0
NORM_EPS = 1e-05


def cond_input(timesteps):
    half_cond = COND // 2
    freqs = jnp.exp(jnp.arange(half_cond, dtype=jnp.float32) * (-math.log(10000.0) / half_cond))
    angles = timesteps.astype(jnp.float32)[:, None] * freqs[None, :]
    return jax.nn.silu(jnp.concatenate([jnp.cos(angles), jnp.sin(angles)], axis=1))


def rotary_tables(positions):
    half_head = HD // 2
    inverse = jnp.exp(jnp.arange(half_head, dtype=jnp.float32) * (-math.log(10000.0) / half_head))
    angles = positions.astype(jnp.float32)[:, None] * inverse[None, :]
    return (jnp.cos(angles), jnp.sin(angles))


def rotate(values, cosines, sines):
    half_head = values.shape[-1] // 2
    first = values[..., :half_head]
    second = values[..., half_head:]
    cos_b = cosines[:, None, :]
    sin_b = sines[:, None, :]
    return jnp.concatenate(
        [first * cos_b - second * sin_b, second * cos_b + first * sin_b], axis=-1
    )


def rotate_back(grads, cosines, sines):
    half_head = grads.shape[-1] // 2
    first = grads[..., :half_head]
    second = grads[..., half_head:]
    cos_b = cosines[:, None, :]
    sin_b = sines[:, None, :]
    return jnp.concatenate(
        [first * cos_b + second * sin_b, second * cos_b - first * sin_b], axis=-1
    )


def normalize(values):
    centre = jnp.mean(values, axis=-1, keepdims=True)
    centred = values - centre
    inverse = lax.rsqrt(jnp.mean(centred * centred, axis=-1, keepdims=True) + NORM_EPS)
    return (centred * inverse, inverse)


def norm_back(normed, inverse, grad):
    return inverse * (
        grad
        - jnp.mean(grad, axis=-1, keepdims=True)
        - normed * jnp.mean(grad * normed, axis=-1, keepdims=True)
    )


def split_kv(block, width):
    seqs, block_rows = (block.shape[0], block.shape[1])
    keys = block[..., :width].reshape(seqs, block_rows, width // HD, HD)
    values = block[..., width:].reshape(seqs, block_rows, width // HD, HD)
    return (keys, values)


def attend_piece(carry, piece, queries, width, factor):
    piece_rows = piece.shape[1]
    size = math.gcd(piece_rows, 512)

    def attend_one_block(index, state):
        running, denom, accum = state
        block = lax.dynamic_slice_in_dim(piece, index * size, size, 1)
        keys, values = split_kv(block, width)
        scores = (
            jnp.einsum("sqhd,skhd->shqk", queries, keys, preferred_element_type=jnp.float32)
            * factor
        )
        highest = jnp.maximum(running, jnp.max(scores, axis=-1))
        shrink = jnp.exp(running - highest)
        weights = jnp.exp(scores - highest[..., None])
        denom = denom * shrink + jnp.sum(weights, axis=-1)
        accum = accum * shrink[..., None] + jnp.einsum(
            "shqk,skhd->shqd",
            weights.astype(jnp.bfloat16),
            values,
            preferred_element_type=jnp.float32,
        )
        return (highest, denom, accum)

    return lax.fori_loop(0, piece_rows // size, attend_one_block, carry)


def block_grads(block, queries, grad_out, logsum, delta, width, factor):
    keys, values = split_kv(block, width)
    scores = (
        jnp.einsum("sqhd,skhd->shqk", queries, keys, preferred_element_type=jnp.float32) * factor
    )
    probs = jnp.exp(scores - logsum[..., None])
    dprobs = jnp.einsum("sqhd,skhd->shqk", grad_out, values, preferred_element_type=jnp.float32)
    dscores = (probs * (dprobs - delta[..., None])).astype(jnp.bfloat16)
    return (keys, probs, dscores)


def query_grads(kv_all, queries, grad_out, logsum, delta, width, factor):
    total_rows = kv_all.shape[1]
    size = math.gcd(total_rows, 512)

    def query_one_block(index, accum):
        block = lax.dynamic_slice_in_dim(kv_all, index * size, size, 1)
        keys, probs, dscores = block_grads(block, queries, grad_out, logsum, delta, width, factor)
        return accum + factor * jnp.einsum(
            "shqk,skhd->sqhd", dscores, keys, preferred_element_type=jnp.float32
        )

    return lax.fori_loop(
        0, total_rows // size, query_one_block, jnp.zeros(queries.shape, jnp.float32)
    )


def key_grads(kv_all, queries, grad_out, logsum, delta, width, factor, count):
    size = math.gcd(count, 512)
    seqs = queries.shape[0]

    def key_one_block(index, accum):
        block = lax.dynamic_slice_in_dim(kv_all, index * size, size, 1)
        keys, probs, dscores = block_grads(block, queries, grad_out, logsum, delta, width, factor)
        grad_vals = jnp.einsum(
            "shqk,sqhd->skhd",
            probs.astype(jnp.bfloat16),
            grad_out,
            preferred_element_type=jnp.float32,
        )
        grad_keys = factor * jnp.einsum(
            "shqk,sqhd->skhd", dscores, queries, preferred_element_type=jnp.float32
        )
        joined = jnp.concatenate(
            [grad_keys.reshape(seqs, size, width), grad_vals.reshape(seqs, size, width)], axis=-1
        )
        return lax.dynamic_update_slice_in_dim(
            accum, jnp.transpose(joined, (1, 0, 2)), index * size, 0
        )

    initial = jnp.zeros((count, seqs, 2 * width), jnp.float32)
    return lax.fori_loop(0, count // size, key_one_block, initial)


def adam_step(weight, grad, first, second, rate, decay_rate):
    new_first = BETA_ONE * first + (1.0 - BETA_ONE) * grad
    new_second = BETA_TWO * second + (1.0 - BETA_TWO) * grad * grad
    fixed_first = new_first / (1.0 - BETA_ONE**STEP)
    fixed_second = new_second / (1.0 - BETA_TWO**STEP)
    new_weight = weight - rate * (
        fixed_first / (jnp.sqrt(fixed_second) + ADAM_EPS) + decay_rate * weight
    )
    return (new_first, new_second, new_weight)


def mod_back(grad_hidden, ln_values, normed, scale_part, gain):
    grad_shift = jnp.sum(grad_hidden, axis=1)
    grad_scale = jnp.sum(grad_hidden * ln_values, axis=1)
    grad_ln = grad_hidden * (1.0 + scale_part)
    grad_gain = jnp.sum(grad_ln * normed, axis=(0, 1))
    return (grad_shift, grad_scale, grad_gain, grad_ln * gain)


def plain(
    tokens_in,
    cotangent,
    timesteps,
    span_start,
    span_len,
    vectors,
    w_ada,
    w_qkv,
    w_attn,
    w_in,
    w_out,
    m_vec,
    v_vec,
    m_ada,
    v_ada,
    m_qkv,
    v_qkv,
    m_attn,
    v_attn,
    m_in,
    v_in,
    m_out,
    v_out,
):
    seqs, group, width = tokens_in.shape
    heads = width // HD
    factor = HD ** (-0.5)
    flat_rows = seqs * group
    full_ada, full_qkv, full_attn, full_in, full_out = (
        lax.all_gather(w_ada.astype(jnp.bfloat16), ("dp", "seq"), axis=1, tiled=True),
        lax.all_gather(w_qkv.astype(jnp.bfloat16), ("dp", "seq"), axis=0, tiled=True),
        lax.all_gather(w_attn.astype(jnp.bfloat16), ("dp", "seq"), axis=0, tiled=True),
        lax.all_gather(w_in.astype(jnp.bfloat16), ("dp", "seq"), axis=0, tiled=True),
        lax.all_gather(w_out.astype(jnp.bfloat16), ("dp", "seq"), axis=0, tiled=True),
    )
    positions = lax.axis_index("seq") * group + jnp.arange(group, dtype=jnp.int32)
    masked = (positions[None, :] >= span_start[:, None]) & (
        positions[None, :] < (span_start + span_len)[:, None]
    )
    cond_bf = cond_input(timesteps).astype(jnp.bfloat16)
    modulation = jnp.dot(cond_bf, full_ada, preferred_element_type=jnp.float32) + vectors[
        2:8
    ].reshape(1, 6 * width)
    pieces = [modulation[:, which * width : (which + 1) * width][:, None, :] for which in range(6)]
    shift_one, scale_one, gate_one, shift_two, scale_two, gate_two = pieces
    start_tokens = jnp.where(
        masked[..., None], vectors[8][None, None, :], tokens_in.astype(jnp.float32)
    )
    normed_one, inv_one = normalize(start_tokens)
    ln_one = normed_one * vectors[0]
    hidden_one = (
        (ln_one * (1.0 + scale_one) + shift_one).astype(jnp.bfloat16).reshape(flat_rows, width)
    )
    projected = jnp.dot(hidden_one, full_qkv, preferred_element_type=jnp.float32).reshape(
        seqs, group, 3 * width
    )
    cosines, sines = rotary_tables(positions)
    queries = rotate(projected[..., :width].reshape(seqs, group, heads, HD), cosines, sines).astype(
        jnp.bfloat16
    )
    keys_here = rotate(
        projected[..., width : 2 * width].reshape(seqs, group, heads, HD), cosines, sines
    ).astype(jnp.bfloat16)
    values_here = projected[..., 2 * width :].astype(jnp.bfloat16)
    kv_local = jnp.concatenate([keys_here.reshape(seqs, group, width), values_here], axis=-1)
    initial = (
        jnp.full((seqs, heads, group), -1e30, jnp.float32),
        jnp.zeros((seqs, heads, group), jnp.float32),
        jnp.zeros((seqs, heads, group, HD), jnp.float32),
    )
    running, denom, accum = attend_piece(
        initial, lax.all_gather(kv_local, "seq", axis=1, tiled=True), queries, width, factor
    )
    attn_heads = accum / denom[..., None]
    logsum = running + jnp.log(denom)
    attn_rows = jnp.transpose(attn_heads, (0, 2, 1, 3)).reshape(flat_rows, width)
    attn_bf = attn_rows.astype(jnp.bfloat16)
    branch_one = jnp.dot(attn_bf, full_attn, preferred_element_type=jnp.float32).reshape(
        seqs, group, width
    )
    mid_tokens = start_tokens + gate_one * branch_one
    normed_two, inv_two = normalize(mid_tokens)
    ln_two = normed_two * vectors[1]
    hidden_two = (
        (ln_two * (1.0 + scale_two) + shift_two).astype(jnp.bfloat16).reshape(flat_rows, width)
    )
    pre_act = jnp.dot(hidden_two, full_in, preferred_element_type=jnp.float32)
    activ, gelu_back = jax.vjp(partial(jax.nn.gelu, approximate=True), pre_act)
    activ_bf = activ.astype(jnp.bfloat16)
    branch_two = jnp.dot(activ_bf, full_out, preferred_element_type=jnp.float32).reshape(
        seqs, group, width
    )
    block_out = (mid_tokens + gate_two * branch_two).astype(jnp.bfloat16)
    grad_y = cotangent.astype(jnp.float32)
    grad_gate_two = jnp.sum(grad_y * branch_two, axis=1)
    grad_branch_two = (grad_y * gate_two).astype(jnp.bfloat16).reshape(flat_rows, width)
    grad_w_out = jnp.dot(activ_bf.T, grad_branch_two, preferred_element_type=jnp.float32)
    grad_activ = jnp.dot(grad_branch_two, full_out.T, preferred_element_type=jnp.float32)
    grad_pre = gelu_back(grad_activ)[0].astype(jnp.bfloat16)
    grad_w_in = jnp.dot(hidden_two.T, grad_pre, preferred_element_type=jnp.float32)
    grad_hidden_two = jnp.dot(grad_pre, full_in.T, preferred_element_type=jnp.float32).reshape(
        seqs, group, width
    )
    grad_shift_two, grad_scale_two, grad_gain_two, grad_normed_two = mod_back(
        grad_hidden_two, ln_two, normed_two, scale_two, vectors[1]
    )
    grad_mid = grad_y + norm_back(normed_two, inv_two, grad_normed_two)
    grad_gate_one = jnp.sum(grad_mid * branch_one, axis=1)
    grad_branch_one = (grad_mid * gate_one).astype(jnp.bfloat16).reshape(flat_rows, width)
    grad_w_attn = jnp.dot(attn_bf.T, grad_branch_one, preferred_element_type=jnp.float32)
    grad_attn_bf = (
        jnp.dot(grad_branch_one, full_attn.T, preferred_element_type=jnp.float32)
        .astype(jnp.bfloat16)
        .reshape(seqs, group, heads, HD)
    )
    delta = jnp.einsum("sqhd,shqd->shq", grad_attn_bf.astype(jnp.float32), attn_heads)
    kv_all = lax.all_gather(kv_local, "seq", axis=1, tiled=True)
    grad_queries = query_grads(kv_all, queries, grad_attn_bf, logsum, delta, width, factor)
    grad_kv = jnp.transpose(
        lax.psum_scatter(
            key_grads(
                kv_all,
                queries,
                grad_attn_bf,
                logsum,
                delta,
                width,
                factor,
                group * lax.axis_size("seq"),
            ).astype(jnp.bfloat16),
            "seq",
            scatter_dimension=0,
            tiled=True,
        ).astype(jnp.float32),
        (1, 0, 2),
    )
    grad_keys = grad_kv[..., :width].reshape(seqs, group, heads, HD)
    grad_qkv = jnp.concatenate(
        [
            rotate_back(grad_queries, cosines, sines).reshape(seqs, group, width),
            rotate_back(grad_keys, cosines, sines).reshape(seqs, group, width),
            grad_kv[..., width:],
        ],
        axis=-1,
    )
    grad_qkv = grad_qkv.astype(jnp.bfloat16).reshape(flat_rows, 3 * width)
    grad_w_qkv = jnp.dot(hidden_one.T, grad_qkv, preferred_element_type=jnp.float32)
    grad_hidden_one = jnp.dot(grad_qkv, full_qkv.T, preferred_element_type=jnp.float32).reshape(
        seqs, group, width
    )
    grad_shift_one, grad_scale_one, grad_gain_one, grad_normed_one = mod_back(
        grad_hidden_one, ln_one, normed_one, scale_one, vectors[0]
    )
    grad_start = grad_mid + norm_back(normed_one, inv_one, grad_normed_one)
    grad_mask_row = jnp.sum(jnp.where(masked[..., None], grad_start, 0.0), axis=(0, 1))
    grad_input = jnp.where(masked[..., None], 0.0, grad_start)
    grad_mod = jnp.concatenate(
        [
            grad_shift_one,
            grad_scale_one,
            grad_gate_one,
            grad_shift_two,
            grad_scale_two,
            grad_gate_two,
        ],
        axis=1,
    )
    grad_w_ada = jnp.dot(cond_bf.astype(jnp.float32).T, grad_mod, precision=lax.Precision.HIGHEST)
    grad_vectors = jnp.concatenate(
        [
            grad_gain_one[None, :],
            grad_gain_two[None, :],
            jnp.sum(grad_mod, axis=0).reshape(6, width),
            grad_mask_row[None, :],
        ],
        axis=0,
    )
    red_ada, red_qkv, red_attn, red_in, red_out, red_vec = (
        lax.psum_scatter(grad_w_ada, ("dp", "seq"), scatter_dimension=1, tiled=True),
        lax.psum_scatter(grad_w_qkv, ("dp", "seq"), scatter_dimension=0, tiled=True),
        lax.psum_scatter(grad_w_attn, ("dp", "seq"), scatter_dimension=0, tiled=True),
        lax.psum_scatter(grad_w_in, ("dp", "seq"), scatter_dimension=0, tiled=True),
        lax.psum_scatter(grad_w_out, ("dp", "seq"), scatter_dimension=0, tiled=True),
        lax.psum_scatter(grad_vectors, ("dp", "seq"), scatter_dimension=1, tiled=True),
    )
    local_squares = jnp.float32(0.0)
    for reduced in (red_vec, red_ada, red_qkv, red_attn, red_in, red_out):
        local_squares = local_squares + jnp.sum(reduced * reduced)
    grad_norm = jnp.sqrt(lax.psum(local_squares, ("dp", "seq")))
    clip_factor = jnp.minimum(1.0, CLIP / (grad_norm + 1e-06))
    columns = red_vec.shape[1]
    own_vectors = lax.dynamic_slice_in_dim(
        vectors, lax.axis_index(("dp", "seq")) * columns, columns, 1
    )
    vec_out = adam_step(own_vectors, red_vec * clip_factor, m_vec, v_vec, RATE_VECTORS, 0.0)
    ada_out = adam_step(w_ada, red_ada * clip_factor, m_ada, v_ada, RATE, DECAY)
    qkv_out = adam_step(w_qkv, red_qkv * clip_factor, m_qkv, v_qkv, RATE, DECAY)
    attn_out = adam_step(w_attn, red_attn * clip_factor, m_attn, v_attn, RATE, DECAY)
    in_out = adam_step(w_in, red_in * clip_factor, m_in, v_in, RATE, DECAY)
    out_out = adam_step(w_out, red_out * clip_factor, m_out, v_out, RATE, DECAY)
    return (
        block_out,
        grad_input,
        grad_norm,
        vec_out[0],
        vec_out[1],
        vec_out[2],
        ada_out[0],
        ada_out[1],
        ada_out[2],
        qkv_out[0],
        qkv_out[1],
        qkv_out[2],
        attn_out[0],
        attn_out[1],
        attn_out[2],
        in_out[0],
        in_out[1],
        in_out[2],
        out_out[0],
        out_out[1],
        out_out[2],
    )


F32, BF = jnp.float32, jnp.bfloat16
MESH = pl.DeviceIdType.MESH
DP, LINE, SEQ, CHIPS, ALL = 4, 4, 8, 16, 32
ROWS, WIDTH, PACK = 128, 768, 640
HALF = WIDTH // 2
HALVES = ((0, 0), (0, 1), (0, 2), (2, 2), (1, 0), (1, 1), (1, 2), None, (2, 0), (2, 1))

def numbered(**counts):
    at = {}
    for name, count in counts.items():
        at[name] = sum(counts[other] for other in at)
    return SimpleNamespace(**at), sum(counts.values())


S, SEM_COUNT = numbered(
    cond=1,
    mix_qkv=1,
    mix_in=1,
    mix_attn=1,
    mod=1,
    w_qkv=1,
    w_attn=1,
    w_in=1,
    w_out=1,
    group_qkv=1,
    group_attn=1,
    fw_qkv=1,
    fw_attn=1,
    fw_in=1,
    fw_out=1,
    tok=4,
    h2=4,
    dm=4,
    xf=4,
    o=1,
    mm=1,
    dh2=1,
    do=1,
    gp=1,
    dh1=1,
    pair_out=1,
    pair_in=1,
    pair_attn=1,
    pair_qkv=1,
    plane_attn=1,
    plane_qkv=1,
    line_out=1,
    line_in=1,
    line_attn=1,
    line_qkv=1,
    last_in=1,
    last_attn=1,
    last_qkv=1,
    early=1,
    early2=1,
    late=1,
    late2=1,
    sq=1,
)

SCRATCH = dict(
    wide_qkv=((48, 3072), F32),
    wide_in=((48, 3072), F32),
    wide_attn=((48, 768), F32),
    s_qkv=((48, 3072), BF),
    s_in=((48, 3072), BF),
    s_attn=((48, 768), BF),
    s_out=((96, 768), BF),
    w_qkv=((768, 768), BF),
    w_in=((768, 768), BF),
    w_attn=((768, 768), BF),
    w_out=((4, 2, 96, 768), BF),
    conds_all=((4, 8, 128), F32),
    mod_send=((4, 4, 128), F32),
    mod_got=((32, 4, 128), F32),
    mod_flat=((40, 128), F32),
    mod_pad=((8, 384), F32),
    turn=((2, 4, 128, 128), F32),
    dmod_flat=((4, 40, 128), F32),
    mod=((8, 768), F32),
    x0=((128, 768), F32),
    n1=((128, 768), F32),
    inv1=((128, 128), F32),
    x1=((128, 768), F32),
    n2=((128, 768), F32),
    inv2=((128, 128), F32),
    a=((128, 768), F32),
    dx1=((128, 768), F32),
    toks=((4, 128, 768), BF),
    h1=((4, 128, 768), BF),
    h2=((4, 128, 768), BF),
    dm=((4, 128, 768), BF),
    gb=((4, 128, 768), BF),
    du=((4, 128, 768), BF),
    xb=((2, 4, 128, 640), BF),
    pt=((3, 1024, 512), BF),
    ot=((2, 128, 512), F32),
    os=((4, 128, 256), BF),
    ob=((4, 128, 256), BF),
    mms=((4, 128, 768), BF),
    mmr=((4, 128, 768), BF),
    dhs=((4, 128, 768), BF),
    dhr=((4, 128, 768), BF),
    das=((128, 768), BF),
    dos=((4, 128, 256), BF),
    dob=((4, 128, 256), BF),
    dst=((3, 1024, 512), BF),
    ga=((512, 640), F32),
    gps=((512, 512), BF),
    gpr=((512, 512), BF),
    dqkv=((4, 128, 768), BF),
    d1s=((4, 128, 768), BF),
    d1r=((4, 128, 768), BF),
    g_out=((4, 2, 96, 768), BF),
    g_in=((2, 768, 384), BF),
    g_attn=((2, 768, 384), BF),
    g_qkv=((2, 768, 384), BF),
    p_out=((4, 96, 768), BF),
    p_in=((768, 384), BF),
    p_attn=((768, 384), BF),
    p_qkv=((768, 384), BF),
    q_attn=((4, 192, 384), BF),
    q_qkv=((4, 192, 384), BF),
    m_attn=((192, 384), BF),
    m_qkv=((192, 384), BF),
    r_out=((4, 96, 768), BF),
    r_in=((16, 48, 384), BF),
    r_attn=((4, 48, 384), BF),
    r_qkv=((4, 48, 384), BF),
    t_in=((4, 48, 384), F32),
    t_attn=((1, 48, 384), F32),
    t_qkv=((4, 48, 384), F32),
    f_in=((4, 2, 24, 384), F32),
    f_attn=((1, 2, 24, 384), F32),
    f_qkv=((4, 2, 24, 384), F32),
    early=((8, 768), F32),
    early_got=((8, 8, 768), F32),
    early_all=((4, 8, 768), F32),
    late=((4, 768), F32),
    late_got=((8, 4, 768), F32),
    late_all=((4, 4, 768), F32),
    sq=((32, 1, 128), F32),
)


def dot(left, right):
    return jnp.dot(left, right, preferred_element_type=F32)


def dot_nt(left, right):
    return lax.dot_general(left, right, (((1,), (1,)), ((), ())), preferred_element_type=F32)


def dot_tn(left, right):
    return lax.dot_general(left, right, (((0,), (0,)), ((), ())), preferred_element_type=F32)


def loop(count, body, start=0):
    def step(index, carry):
        body(index)
        return carry

    lax.fori_loop(start, count, step, 0)


def layer_kernel(
    i_time,
    i_start,
    i_len,
    i_tok,
    i_cot,
    i_vec,
    i_wada,
    i_wqkv,
    i_wattn,
    i_win,
    i_wout,
    o_y,
    o_dx,
    o_norm,
    o_gqkv,
    o_gattn,
    o_gin,
    o_gout,
    o_dmod,
    o_gvec,
    o_vec,
    o_conds,
    *scratch,
):
    r = SimpleNamespace(**dict(zip(SCRATCH, scratch)))
    send_sems, recv_sems = scratch[-2:]
    b, s = lax.axis_index("dp"), lax.axis_index("seq")
    z, c = lax.div(s, 2), lax.rem(s, 2)
    mate = s + 1 - 2 * c
    chip = b * LINE + z
    me = b * SEQ + s
    drains = []

    def push(src, dst, at, to_b, to_s):
        pltpu.make_async_remote_copy(
            src_ref=src,
            dst_ref=dst,
            send_sem=send_sems.at[at],
            recv_sem=recv_sems.at[at],
            device_id=(to_b, to_s),
            device_id_type=MESH,
        ).start()

    def keep(src, dst, at):
        pltpu.make_async_copy(src, dst, recv_sems.at[at]).start()

    def got(at, like):
        pltpu.make_async_copy(like, like, recv_sems.at[at]).wait()

    def left(at, like):
        pltpu.make_async_copy(like, like, send_sems.at[at]).wait()

    def sent(at, like):
        drains.append((at, like))

    near = (b, b + 1 - 2 * lax.rem(b, 2), b + 2 - 4 * lax.div(b, 2), 3 - b)

    def peers(body):
        for k in (1, 2, 3):
            body(k, near[k])

    def stack(body):
        for k in (1, 2, 3):
            body(lax.rem(z + k, LINE))

    lane = lax.broadcasted_iota(jnp.int32, (1, 128), 1)
    low = lane < 64
    own24 = pl.ds(pl.multiple_of(24 * c, 8), 24)
    mate24 = pl.ds(pl.multiple_of(24 * (1 - c), 8), 24)
    part = pl.ds(pl.multiple_of(HALF * c, 128), HALF)
    chip_rows = pl.ds(pl.multiple_of(48 * chip, 16), 48)
    group_rows = pl.ds(pl.multiple_of(192 * b, 16), 192)

    barrier = pltpu.get_barrier_semaphore()

    def greet(k):
        other = lax.rem(me + k, ALL)
        pl.semaphore_signal(
            barrier, inc=1, device_id=(lax.div(other, SEQ), lax.rem(other, SEQ)), device_id_type=MESH
        )

    loop(ALL, greet, 1)

    def natural(kind, p, head):
        return kind * WIDTH + 192 * p + 64 * head

    def half_at(ref, column, high):
        tile = ref[:, column // 128 * 128 : column // 128 * 128 + 128]
        return tile if (column % 128 == 64) == high else pltpu.roll(tile, 64, 1)

    for p in range(4):
        for tile in range(5):
            pair = []
            for high in (0, 1):
                which = HALVES[2 * tile + high]
                pair.append(
                    jnp.zeros((24, 128), F32)
                    if which is None
                    else half_at(i_wqkv, natural(which[0], p, which[1]), bool(high))
                )
            r.wide_qkv[own24, 768 * p + 128 * tile : 768 * p + 128 * tile + 128] = jnp.where(
                low, pair[0], pair[1]
            )
        r.wide_qkv[own24, 768 * p + 640 : 768 * p + 768] = jnp.zeros((24, 128), F32)
    r.wide_in[own24, :] = i_win[...]
    r.wide_attn[own24, :] = i_wattn[...]
    r.s_out[...] = i_wout[...].astype(BF)
    lanes8 = lax.broadcasted_iota(jnp.int32, (8, 128), 1)
    half_cond = COND // 2
    speed = jnp.exp((lanes8 % half_cond).astype(F32) * (-math.log(10000.0) / half_cond))
    angle = i_time[0].astype(F32) * speed
    wave = jnp.where(lanes8 < half_cond, jnp.cos(angle), jnp.sin(angle))
    r.conds_all[b] = wave * (1.0 / (1.0 + jnp.exp(-wave)))
    pl.semaphore_wait(barrier, ALL - 1)

    def stack_rows(to):
        push(r.s_out, r.w_out.at[z, c], S.w_out, b, 2 * to + c)

    peers(lambda k, to: push(r.conds_all.at[b], r.conds_all.at[b], S.cond, to, s))
    sent(S.cond, r.conds_all.at[0:3])
    stack(lambda to: push(i_tok.at[0], r.toks.at[z], S.tok + z, b, 2 * to + c))
    sent(S.tok + z, r.toks.at[0:3])
    push(r.wide_qkv.at[own24], r.wide_qkv.at[own24], S.mix_qkv, b, mate)
    sent(S.mix_qkv, r.wide_qkv.at[0:24])
    push(r.wide_attn.at[own24], r.wide_attn.at[own24], S.mix_attn, b, mate)
    sent(S.mix_attn, r.wide_attn.at[0:24])
    push(r.wide_in.at[own24], r.wide_in.at[own24], S.mix_in, b, mate)
    sent(S.mix_in, r.wide_in.at[0:24])

    got(S.cond, r.conds_all.at[0:3])
    row8 = lax.broadcasted_iota(jnp.int32, (8, 128), 0)
    cond4 = jnp.zeros((8, 128), F32)
    for k in range(4):
        cond4 = jnp.where(row8 == k, r.conds_all[k], cond4)
    o_conds[...] = cond4
    wide = i_wada.shape[0]
    r.mod_pad[...] = jnp.zeros((8, 384), F32)
    r.mod_pad[:, 0:wide] = dot_nt(cond4.astype(BF), i_wada[...].astype(BF))
    columns = pltpu.roll(r.mod_pad[...], lax.rem(wide * me, 128), 1)
    for k in range(4):
        for t in range(3):
            r.mod_send[k, t : t + 1, :] = columns[k : k + 1, 128 * t : 128 * t + 128]
        r.mod_send[k, 3:4, :] = jnp.zeros((1, 128), F32)

    def send_mod(k):
        other = lax.rem(me + k, ALL)
        ob = lax.div(other, SEQ)
        push(r.mod_send.at[ob], r.mod_got.at[me], S.mod, ob, lax.rem(other, SEQ))

    loop(ALL, send_mod, 1)
    sent(S.mod, r.mod_got.at[0:31])
    keep(r.mod_send.at[b], r.mod_got.at[me], S.mod)

    def block(src, first):
        return src.at[:, pl.ds(pl.multiple_of(first, 128), HALF)]

    def spread(src, dst, at):
        def one(k):
            to = lax.rem(chip + k, CHIPS)
            to_b, to_z = lax.div(to, LINE), lax.rem(to, LINE)
            push(
                block(src, WIDTH * to_b + HALF * c),
                dst.at[chip_rows, part],
                at,
                to_b,
                2 * to_z + c,
            )

        loop(CHIPS, one, 1)
        keep(block(src, WIDTH * b + HALF * c), dst.at[chip_rows, part], at)
        sent(at, dst.at[0:720, 0:HALF])

    def along_line(src, dst, at, step):
        stack(
            lambda to: push(
                block(src, step * to + HALF * c), dst.at[chip_rows, part], at, b, 2 * to + c
            )
        )
        keep(block(src, step * z + HALF * c), dst.at[chip_rows, part], at)
        sent(at, dst.at[0:144, 0:HALF])

    def over_plane(dst, first, at):
        got(first, dst.at[0:192, 0:HALF])
        peers(
            lambda k, to: push(dst.at[group_rows, part], dst.at[group_rows, part], at, to, s)
        )
        sent(at, dst.at[0:576, 0:HALF])

    def share(dst, at, onward, rows):
        got(at, dst.at[0:rows, 0:HALF])
        push(dst.at[:, part], dst.at[:, part], onward, b, mate)
        sent(onward, dst.at[:, 0:HALF])

    got(S.mix_qkv, r.wide_qkv.at[0:24])
    r.s_qkv[...] = r.wide_qkv[...].astype(BF)
    along_line(r.s_qkv, r.w_qkv, S.w_qkv, WIDTH)
    got(S.mix_attn, r.wide_attn.at[0:24])
    r.s_attn[...] = r.wide_attn[...].astype(BF)
    along_line(r.s_attn, r.w_attn, S.w_attn, 0)

    def start_tokens(tokens, k):
        place = (2 * k + c) * ROWS + lax.broadcasted_iota(jnp.int32, (ROWS, 1), 0)
        hidden = (place >= i_start[0]) & (place < i_start[0] + i_len[0])
        return jnp.where(hidden, i_vec[8:9, :], tokens.astype(F32)), hidden

    x0, _ = start_tokens(i_tok[0], z)
    r.x0[...] = x0
    n1, inv1 = normalize(x0)
    r.n1[...] = n1
    r.inv1[...] = jnp.broadcast_to(inv1, (ROWS, 128))

    got(S.mod, r.mod_got)
    r.mod_flat[...] = jnp.zeros((40, 128), F32)
    for k in range(ALL):
        first = 9 * k // 8
        r.mod_flat[first : first + 3, :] += r.mod_got[k, 0:3, :]
    for k in range(6):
        row = jnp.concatenate(
            [r.mod_flat[6 * k + t : 6 * k + t + 1, :] for t in range(6)], axis=1
        )
        r.mod[k : k + 1, :] = row + i_vec[2 + k : 3 + k, :]

    def mod(k):
        return r.mod[k : k + 1, :]

    def vec(k):
        return i_vec[k : k + 1, :]

    r.h1[z] = (r.n1[...] * vec(0) * (1.0 + mod(1)) + mod(0)).astype(BF)
    r.dm[0] = (i_cot[0].astype(F32) * mod(5)).astype(BF)
    over_plane(r.w_qkv, S.w_qkv, S.group_qkv)
    peers(lambda k, to: push(r.dm.at[0], r.dm.at[k], S.dm + k, to, s))
    for k in (1, 2, 3):
        sent(S.dm + k, r.dm.at[0])

    lanes = lax.broadcasted_iota(jnp.int32, (ROWS, 128), 1)
    first_half = lanes % HD < HD // 2
    speed = jnp.exp((lanes % (HD // 2)).astype(F32) * (-math.log(10000.0) / (HD // 2)))
    row = lax.broadcasted_iota(jnp.int32, (ROWS, 128), 0)

    def table(k):
        angle = ((2 * k + c) * ROWS + row).astype(F32) * speed
        r.turn[0, k] = jnp.cos(angle)
        sine = jnp.sin(angle)
        r.turn[1, k] = jnp.where(first_half, -sine, sine)

    loop(LINE, table)

    got(S.mix_in, r.wide_in.at[0:24])
    r.s_in[...] = r.wide_in[...].astype(BF)

    share(r.w_qkv, S.group_qkv, S.fw_qkv, 576)
    over_plane(r.w_attn, S.w_attn, S.group_attn)
    got(S.fw_qkv, r.w_qkv.at[:, 0:HALF])

    def turned(tile, sign, k):
        other = jnp.where(first_half, pltpu.roll(tile, 96, 1), pltpu.roll(tile, 32, 1))
        return tile * r.turn[0, k] + sign * (other * r.turn[1, k])

    def project(j):
        k = lax.rem(z + j, LINE)

        @pl.when(j > 0)
        def _():
            got(S.tok + k, r.toks.at[0])
            other, _ = start_tokens(r.toks[k], k)
            other, _ = normalize(other)
            r.h1[k] = (other * vec(0) * (1.0 + mod(1)) + mod(0)).astype(BF)

        x = dot(r.h1[k], r.w_qkv[:, 0:PACK])
        tiles = [x[:, 128 * t : 128 * t + 128] for t in range(5)]
        tiles[0] = turned(tiles[0], 1.0, k) * 0.125
        tiles[1] = jnp.where(low, turned(tiles[1], 1.0, k) * 0.125, tiles[1])
        tiles[2] = turned(tiles[2], 1.0, k)
        tiles[3] = turned(tiles[3], 1.0, k)
        for t in range(5):
            r.xb[0, k, :, 128 * t : 128 * t + 128] = tiles[t].astype(BF)
        push(r.xb.at[0, k], r.xb.at[1, k], S.xf + k, b, mate)

    loop(4, project)
    for k in range(4):
        sent(S.xf + k, r.xb.at[0, 0])

    stack(stack_rows)
    keep(r.s_out, r.w_out.at[z, c], S.w_out)
    sent(S.w_out, r.w_out.at[0:3, 0])
    spread(r.s_in, r.w_in, S.w_in)
    for k in range(4):
        got(S.xf + k, r.xb.at[0, 0])

    def tile_of(t):
        return r.xb[:, :, :, 128 * t : 128 * t + 128].reshape(1024, 128)

    heads = ((0, 2, 4, True, True), (0, 2, 4, False, False), (1, 3, 1, True, False))

    def queries(head, first, size):
        q_tile, _, _, q_low, _ = heads[head]
        q = r.xb[0, first : first + size, :, 128 * q_tile : 128 * q_tile + 128]
        return jnp.where(low if q_low else ~low, q.reshape(size * 128, 128), jnp.zeros((), BF))

    for half in range(2):
        at = slice(256 * half, 256 * half + 256)
        for head in range(3):
            scores = dot_nt(tile_of(heads[head][1]), queries(head, 2 * half, 2))
            weights = jnp.exp(scores - jnp.max(scores, axis=0, keepdims=True))
            weights = weights * (1.0 / jnp.sum(weights, axis=0, keepdims=True))
            weights = weights.astype(BF)
            r.pt[head, :, at] = weights
            out = dot_tn(tile_of(heads[head][2]), weights)
            if head == 0:
                r.ot[0, 0:64, at] = out[0:64]
            elif head == 1:
                r.ot[0, 64:128, at] = out[64:128]
            else:
                r.ot[1, 0:64, at] = out[64:128]
                r.ot[1, 64:128, at] = jnp.zeros((64, 256), F32)
        for t in range(2):
            r.os[2 * half : 2 * half + 2, :, 128 * t : 128 * t + 128] = (
                r.ot[t, :, at].T.astype(BF).reshape(2, 128, 128)
            )
        for to in (2 * half, 2 * half + 1):

            @pl.when(z == to)
            def _():
                keep(r.os.at[to], r.ob.at[z], S.o)

            @pl.when(z != to)
            def _():
                push(r.os.at[to], r.ob.at[z], S.o, b, 2 * to + c)

    sent(S.o, r.os.at[0:3])
    share(r.w_attn, S.group_attn, S.fw_attn, 576)
    got(S.fw_attn, r.w_attn.at[:, 0:HALF])
    got(S.o, r.ob)
    a = jnp.zeros((ROWS, WIDTH), F32)
    for p in range(4):
        a += dot(r.ob[p, :, 0:128], r.w_attn[192 * p : 192 * p + 128, :])
        a += dot(r.ob[p, :, 128:192], r.w_attn[192 * p + 128 : 192 * p + 192, :])
    r.a[...] = a
    x1 = r.x0[...] + mod(2) * a
    r.x1[...] = x1
    n2, inv2 = normalize(x1)
    r.n2[...] = n2
    r.inv2[...] = jnp.broadcast_to(inv2, (ROWS, 128))
    r.h2[0] = (n2 * vec(1) * (1.0 + mod(4)) + mod(3)).astype(BF)
    peers(lambda k, to: push(r.h2.at[0], r.h2.at[k], S.h2 + k, to, s))
    for k in (1, 2, 3):
        sent(S.h2 + k, r.h2.at[0])
    got(S.w_out, r.w_out.at[:, 0])
    push(r.w_out.at[:, c], r.w_out.at[:, c], S.fw_out, b, mate)
    sent(S.fw_out, r.w_out.at[:, 0])
    share(r.w_in, S.w_in, S.fw_in, 768)
    got(S.fw_out, r.w_out.at[:, 0])
    got(S.fw_in, r.w_in.at[:, 0:HALF])

    def feed(k):
        @pl.when(k > 0)
        def _():
            got(S.h2 + k, r.h2.at[0])
            got(S.dm + k, r.dm.at[0])

        u = dot(r.h2[k], r.w_in[...])
        slope = 0.7978845608028654
        cube = 0.044715
        t = jnp.tanh(slope * (u + cube * u * u * u))
        r.gb[k] = (0.5 * u * (1.0 + t)).astype(BF)
        bend = 0.5 * (1.0 + t) + 0.5 * u * (1.0 - t * t) * (slope * (1.0 + 3.0 * cube * u * u))
        r.du[k] = (dot_nt(r.dm[k], r.w_out[...].reshape(WIDTH, WIDTH)) * bend).astype(BF)
        r.dhs[k] = dot_nt(r.du[k], r.w_in[...]).astype(BF)
        for n in (1, 2, 3):

            @pl.when(k == n)
            def _():
                push(r.dhs.at[n], r.dhr.at[n], S.dh2, near[n], s)

    loop(4, feed)
    sent(S.dh2, r.dhs.at[0:3])

    def feed_out(k):
        r.mms[k] = dot(r.gb[k], r.w_out[...].reshape(WIDTH, WIDTH)).astype(BF)

    loop(4, feed_out)
    peers(lambda k, to: push(r.mms.at[k], r.mmr.at[k], S.mm, to, s))
    sent(S.mm, r.mms.at[0:3])

    def gather(own, others):
        total = own[0].astype(F32)
        for k in (1, 2, 3):
            total += others[k].astype(F32)
        return total

    for k in range(4):
        rows = slice(192 * k, 192 * k + 192)
        block = dot_tn(r.gb[:, :, rows].reshape(512, 192), r.dm[...].reshape(512, 768))
        r.g_out[k] = block.astype(BF).reshape(2, 96, 768)
    push(r.g_out.at[:, 1 - c], r.p_out, S.pair_out, b, mate)
    sent(S.pair_out, r.p_out)

    def outer(left, right, dst):
        def one(k):
            rows = pl.ds(pl.multiple_of(128 * k, 128), 128)
            result = dot_tn(
                left[:, :, rows].reshape(512, 128), right[...].reshape(512, 768)
            ).astype(BF)
            dst[0, rows, :] = result[:, 0:HALF]
            dst[1, rows, :] = result[:, HALF:WIDTH]

        loop(6, one)

    def to_mate(grad, dst, at):
        push(grad.at[1 - c], dst, at, b, mate)
        sent(at, dst)

    def pair_sum(grad, pair, at):
        got(at, pair)
        grad[c] = (grad[c].astype(F32) + pair[...].astype(F32)).astype(BF)

    def plane_sum(grad, dst, at):
        def rows(to):
            return grad.at[c, pl.ds(pl.multiple_of(192 * to, 16), 192)]

        peers(lambda k, to: push(rows(to), dst.at[k], at, to, s))
        keep(rows(b), dst.at[0], at)
        sent(at, dst.at[0:3])

    def line_sum(src, total, dst, first, at):
        got(first, src)
        total[...] = (
            (src[0].astype(F32) + src[1].astype(F32)) + (src[2].astype(F32) + src[3].astype(F32))
        ).astype(BF)

        def rows(to):
            return total.at[pl.ds(pl.multiple_of(48 * to, 16), 48)]

        stack(lambda to: push(rows(to), dst.at[z], at, b, 2 * to + c))
        keep(rows(z), dst.at[z], at)
        sent(at, dst.at[0:3])

    def trade(total, final, at):
        push(total.at[:, mate24], final.at[:, c], at, b, mate)
        sent(at, final.at[:, 0])
        final[:, c] = total[:, own24, :]

    outer(r.h2, r.du, r.g_in)
    to_mate(r.g_in, r.p_in, S.pair_in)

    got(S.pair_out, r.p_out)
    for k in range(4):
        r.g_out[k, c] = (r.g_out[k, c].astype(F32) + r.p_out[k].astype(F32)).astype(BF)

    def send_gout(to):
        push(r.g_out.at[to, c], r.r_out.at[z], S.line_out, b, 2 * to + c)

    stack(send_gout)
    keep(r.g_out.at[z, c], r.r_out.at[z], S.line_out)
    sent(S.line_out, r.r_out.at[0:3])

    got(S.dh2, r.dhr.at[0:3])
    dh = gather(r.dhs, r.dhr)
    n2 = r.n2[...]
    inv2 = r.inv2[:, 0:1]
    r.early[...] = jnp.zeros((8, 768), F32)
    r.early[2:3, :] = jnp.sum(dh, axis=0, keepdims=True)
    both = jnp.sum(dh * n2, axis=0, keepdims=True)
    r.early[3:4, :] = both * vec(1)
    r.early[0:1, :] = both * (1.0 + mod(4))
    grad = dh * ((1.0 + mod(4)) * vec(1))
    dx1 = i_cot[0].astype(F32) + norm_back(n2, inv2, grad)
    r.dx1[...] = dx1
    r.early[1:2, :] = jnp.sum(dx1 * r.a[...], axis=0, keepdims=True)
    r.das[...] = (dx1 * mod(2)).astype(BF)
    for p in range(4):
        first = 192 * p
        r.dos[p, :, 0:128] = dot_nt(r.das[...], r.w_attn[first : first + 128, :]).astype(BF)
        tail = dot_nt(r.das[...], r.w_attn[first + 128 : first + 192, :])
        r.dos[p, :, 128:256] = jnp.concatenate(
            [tail, jnp.zeros((ROWS, 64), F32)], axis=1
        ).astype(BF)

    stack(lambda to: push(r.dos.at[to], r.dob.at[z], S.do, b, 2 * to + c))
    keep(r.dos.at[z], r.dob.at[z], S.do)
    sent(S.do, r.dos.at[0:3])

    for p in range(4):
        rows = slice(192 * p, 192 * p + 192)
        result = dot_tn(r.ob[p], r.das[...])[0:192].astype(BF)
        r.g_attn[0, rows, :] = result[:, 0:HALF]
        r.g_attn[1, rows, :] = result[:, HALF:WIDTH]
    to_mate(r.g_attn, r.p_attn, S.pair_attn)

    got(S.mm, r.mmr.at[0:3])
    mm = gather(r.mms, r.mmr)
    o_y[...] = (r.x1[...] + mod(5) * mm).astype(BF)
    r.early[4:5, :] = jnp.sum(i_cot[0].astype(F32) * mm, axis=0, keepdims=True)

    def over_line(src, dst, name):
        def one(k):
            push(src, dst.at[s], name, b, lax.rem(s + k, SEQ))

        loop(SEQ, one, 1)
        keep(src, dst.at[s], name)
        sent(name, dst.at[0:7])

    def over_group(got_ref, dst, name):
        total = got_ref[0]
        for k in range(1, SEQ):
            total += got_ref[k]
        dst[b] = total
        peers(lambda k, to: push(dst.at[b], dst.at[b], name, to, s))
        sent(name, dst.at[0:3])

    over_line(r.early, r.early_got, S.early)

    pair_sum(r.g_in, r.p_in, S.pair_in)

    def send_gin(k):
        to = lax.rem(chip + k, CHIPS)
        push(
            r.g_in.at[c, pl.ds(pl.multiple_of(48 * to, 16), 48)],
            r.r_in.at[chip],
            S.line_in,
            lax.div(to, LINE),
            2 * lax.rem(to, LINE) + c,
        )

    loop(CHIPS, send_gin, 1)
    keep(r.g_in.at[c, chip_rows], r.r_in.at[chip], S.line_in)
    sent(S.line_in, r.r_in.at[0:15])
    pair_sum(r.g_attn, r.p_attn, S.pair_attn)
    plane_sum(r.g_attn, r.q_attn, S.plane_attn)

    got(S.do, r.dob)
    dot0, dot1 = r.dob[:, :, 0:128].reshape(512, 128), r.dob[:, :, 128:256].reshape(512, 128)
    zero = jnp.zeros((), BF)
    moved = pltpu.roll(dot1.astype(F32), 64, 1).astype(BF)
    grads = (jnp.where(low, dot0, zero), jnp.where(low, zero, dot0), moved)
    product = dot0.astype(F32).T * r.ot[0]
    deltas = (
        jnp.sum(product[0:64], axis=0, keepdims=True),
        jnp.sum(product[64:128], axis=0, keepdims=True),
        jnp.sum(dot1.astype(F32).T * r.ot[1], axis=0, keepdims=True),
    )
    for head in range(3):
        values = tile_of(heads[head][2])
        for half in range(2):
            at = slice(256 * half, 256 * half + 256)
            dp = dot_nt(values, grads[head][at])
            r.dst[head, :, at] = (
                r.pt[head, :, at].astype(F32) * (dp - deltas[head][:, at])
            ).astype(BF)

    def key_grads(rows):
        dk = [dot(r.dst[head, rows, :], queries(head, 0, 4)) for head in range(3)]
        dv = [dot(r.pt[head, rows, :], grads[head]) for head in range(3)]
        return (dv[2], dk[0] + dk[1], dk[2], dv[0] + dv[1])

    for t, tile in enumerate(key_grads(slice(512, 1024))):
        r.gps[:, 128 * t : 128 * t + 128] = tile.astype(BF)
    push(r.gps, r.gpr, S.gp, b, mate)
    sent(S.gp, r.gps)
    for t, tile in enumerate(key_grads(slice(0, 512))):
        r.ga[:, 128 * t + 128 : 128 * t + 256] = tile
    for half in range(2):
        at = slice(256 * half, 256 * half + 256)
        turned_q = [dot_tn(tile_of(heads[head][1]), r.dst[head, :, at]) for head in range(3)]
        top = jnp.concatenate([turned_q[0][0:64], turned_q[1][64:128]], axis=0)
        r.ga[at, 0:128] = top.T * 0.125
        r.ga[at, 128:256] += turned_q[2].T * 0.125
    got(S.gp, r.gpr)

    def unproject(j):
        k = lax.rem(z + 1 + j, LINE)
        rows = pl.ds(pl.multiple_of(128 * k, 128), 128)
        tiles = [r.ga[rows, 0:128]] + [
            r.ga[rows, 128 * t : 128 * t + 128]
            + r.gpr[rows, 128 * t - 128 : 128 * t].astype(F32)
            for t in range(1, 5)
        ]
        tiles[0] = turned(tiles[0], -1.0, k)
        tiles[1] = jnp.where(low, turned(tiles[1], -1.0, k), tiles[1])
        tiles[2] = turned(tiles[2], -1.0, k)
        tiles[3] = turned(tiles[3], -1.0, k)
        for t in range(5):
            r.dqkv[k, :, 128 * t : 128 * t + 128] = tiles[t].astype(BF)
        r.dqkv[k, :, PACK:WIDTH] = jnp.zeros((128, 128), BF)
        r.d1s[k] = dot_nt(r.dqkv[k, :, 0:PACK], r.w_qkv[:, 0:PACK]).astype(BF)

        @pl.when(j < 3)
        def _():
            push(r.d1s.at[k], r.d1r.at[z], S.dh1, b, 2 * k + c)

    loop(4, unproject)
    sent(S.dh1, r.d1s.at[0:3])
    outer(r.h1, r.dqkv, r.g_qkv)
    to_mate(r.g_qkv, r.p_qkv, S.pair_qkv)
    line_sum(r.q_attn, r.m_attn, r.r_attn, S.plane_attn, S.line_attn)
    got(S.early, r.early_got)
    over_group(r.early_got, r.early_all, S.early2)
    pair_sum(r.g_qkv, r.p_qkv, S.pair_qkv)
    plane_sum(r.g_qkv, r.q_qkv, S.plane_qkv)

    got(S.line_in, r.r_in)
    for p in range(4):
        r.t_in[p] = (r.r_in[4 * p].astype(F32) + r.r_in[4 * p + 1].astype(F32)) + (
            r.r_in[4 * p + 2].astype(F32) + r.r_in[4 * p + 3].astype(F32)
        )
    trade(r.t_in, r.f_in, S.last_in)
    line_sum(r.q_qkv, r.m_qkv, r.r_qkv, S.plane_qkv, S.line_qkv)

    got(S.dh1, r.d1r.at[0:3])
    dh = r.d1s[z].astype(F32)
    for k in (1, 2, 3):
        dh += r.d1r[lax.rem(z + k, LINE)].astype(F32)
    n1 = r.n1[...]
    both = jnp.sum(dh * n1, axis=0, keepdims=True)
    r.late[0:1, :] = both * (1.0 + mod(1))
    r.late[1:2, :] = jnp.sum(dh, axis=0, keepdims=True)
    r.late[2:3, :] = both * vec(0)
    grad = dh * ((1.0 + mod(1)) * vec(0))
    dx0 = r.dx1[...] + norm_back(n1, r.inv1[:, 0:1], grad)
    _, hidden = start_tokens(i_tok[0], z)
    o_dx[...] = jnp.where(hidden, 0.0, dx0)
    r.late[3:4, :] = jnp.sum(jnp.where(hidden, dx0, 0.0), axis=0, keepdims=True)
    over_line(r.late, r.late_got, S.late)

    got(S.line_out, r.r_out)
    total = (r.r_out[0].astype(F32) + r.r_out[1].astype(F32)) + (
        r.r_out[2].astype(F32) + r.r_out[3].astype(F32)
    )
    o_gout[...] = total
    squares = total * total
    squares = jnp.sum(squares[:, 0:128] + squares[:, 128:256] + squares[:, 256:384]
                      + squares[:, 384:512] + squares[:, 512:640] + squares[:, 640:768],
                      axis=0, keepdims=True)

    def fold(value):
        total = value[:, 0:128] * value[:, 0:128]
        for t in range(1, value.shape[1] // 128):
            total += value[:, 128 * t : 128 * t + 128] * value[:, 128 * t : 128 * t + 128]
        return jnp.sum(total, axis=0, keepdims=True)

    got(S.line_attn, r.r_attn)
    r.t_attn[0] = (r.r_attn[0].astype(F32) + r.r_attn[1].astype(F32)) + (
        r.r_attn[2].astype(F32) + r.r_attn[3].astype(F32)
    )
    trade(r.t_attn, r.f_attn, S.last_attn)
    got(S.line_qkv, r.r_qkv)
    r.t_qkv[...] = r.r_qkv[...].astype(F32)
    trade(r.t_qkv, r.f_qkv, S.last_qkv)
    got(S.late, r.late_got)
    over_group(r.late_got, r.late_all, S.late2)
    got(S.last_in, r.f_in.at[:, 0])
    got(S.last_attn, r.f_attn.at[:, 0])
    for h in range(2):
        for p in range(4):
            value = r.f_in[p, h]
            o_gin[:, 768 * p + 384 * h : 768 * p + 384 * h + 384] = value
            squares += fold(value)
        value = r.f_attn[0, h]
        o_gattn[:, 384 * h : 384 * h + 384] = value
        squares += fold(value)
    got(S.last_qkv, r.f_qkv.at[:, 0])
    where = {which: index for index, which in enumerate(HALVES) if which is not None}

    def packed_half(chunk, high):
        kind, rest = chunk // 12, chunk % 12
        index = where[(kind, rest % 3)]
        t = index // 2
        tile = r.f_qkv[rest // 3, t // 3, :, t % 3 * 128 : t % 3 * 128 + 128]
        return tile if index % 2 == high else pltpu.roll(tile, 64, 1)

    for t in range(18):
        o_gqkv[:, 128 * t : 128 * t + 128] = jnp.where(
            low, packed_half(2 * t, 0), packed_half(2 * t + 1, 1)
        )
    for p in range(4):
        for h in range(2):
            squares += fold(r.f_qkv[p, h])

    r.sq[me] = squares

    def send_sq(k):
        other = lax.rem(me + k, ALL)
        push(r.sq.at[me], r.sq.at[me], S.sq, lax.div(other, SEQ), lax.rem(other, SEQ))

    loop(ALL, send_sq, 1)
    sent(S.sq, r.sq.at[0:31])
    got(S.early2, r.early_all.at[0:3])
    got(S.late2, r.late_all.at[0:3])
    mods = []
    for k in range(4):
        early, late = r.early_all[k], r.late_all[k]
        rows = jnp.concatenate([late[1:3], early[1:5], jnp.zeros((2, 768), F32)], axis=0)
        for n in range(6):
            for m in range(6):
                r.dmod_flat[k, 6 * n + m : 6 * n + m + 1, :] = rows[
                    n : n + 1, 128 * m : 128 * m + 128
                ]
        mods.append(rows)
    gain = jnp.concatenate(
        [
            sum(r.late_all[k][0:1] for k in range(4)),
            sum(r.early_all[k][0:1] for k in range(4)),
            (mods[0] + mods[1] + mods[2] + mods[3])[0:6],
        ],
        axis=0,
    )
    mask_row = sum(r.late_all[k][3:4] for k in range(4))
    gains = jnp.concatenate([gain, mask_row, jnp.zeros((7, 768), F32)], axis=0)
    masters = jnp.concatenate([i_vec[...], jnp.zeros((7, 768), F32)], axis=0)
    own = lax.rem(WIDTH - 24 * me, WIDTH)
    o_gvec[...] = pltpu.roll(gains, own, 1)[:, 0:128]
    o_vec[...] = pltpu.roll(masters, own, 1)[:, 0:128]
    r.mod_pad[...] = jnp.zeros((8, 384), F32)
    window = lax.div(wide * me, 128)
    for k in range(4):
        rows = r.dmod_flat[k, pl.ds(window, 3), :]
        for m in range(3):
            r.mod_pad[k : k + 1, 128 * m : 128 * m + 128] = rows[m : m + 1, :]
    o_dmod[...] = pltpu.roll(r.mod_pad[...], lax.rem(384 - lax.rem(wide * me, 128), 384), 1)[:, 0:256]
    small = jnp.sum(gain * gain) + jnp.sum(mask_row * mask_row)
    conds = [r.conds_all[k][0:1].astype(BF).astype(F32) for k in range(4)]
    for k in range(4):
        for m in range(k, 4):
            term = jnp.sum(mods[k] * mods[m]) * jnp.sum(conds[k] * conds[m])
            small += term if m == k else 2.0 * term
    got(S.sq, r.sq.at[0:31])
    total = r.sq[0]
    for k in range(1, ALL):
        total += r.sq[k]
    o_norm[...] = jnp.broadcast_to(jnp.sqrt(jnp.sum(total) + small), (8, 128))

    for at, like in drains:
        left(at, like)


def run_layer(*args):
    shapes = (
        ((ROWS, WIDTH), BF),
        ((ROWS, WIDTH), F32),
        ((8, 128), F32),
        ((24, 3 * WIDTH), F32),
        ((24, WIDTH), F32),
        ((24, 4 * WIDTH), F32),
        ((96, WIDTH), F32),
        ((8, 256), F32),
        ((16, 128), F32),
        ((16, 128), F32),
        ((8, 128), F32),
    )
    whole = pl.BlockSpec(memory_space=pltpu.VMEM)
    scalar = pl.BlockSpec(memory_space=pltpu.SMEM)
    return pl.pallas_call(
        layer_kernel,
        out_shape=[jax.ShapeDtypeStruct(shape, kind) for shape, kind in shapes],
        in_specs=[scalar] * 3 + [whole] * (len(args) - 3),
        out_specs=[whole] * len(shapes),
        scratch_shapes=[pltpu.VMEM(shape, kind) for shape, kind in SCRATCH.values()]
        + [pltpu.SemaphoreType.DMA((SEM_COUNT,)), pltpu.SemaphoreType.DMA((SEM_COUNT,))],
        compiler_params=pltpu.CompilerParams(
            collective_id=0, has_side_effects=True, vmem_limit_bytes=60 * 1024 * 1024
        ),
    )(*args)


def finish_kernel(
    y, dx, norm, g_qkv, g_attn, g_in, g_out, dmod, g_vec, own_vec, conds, *rest
):
    (w_ada, w_qkv, w_attn, w_in, w_out), moments, outs = rest[:5], rest[5:17], rest[17:]
    outs[0][0] = y[...]
    outs[1][0] = dx[...]
    outs[2][0, 0] = norm[0, 0]
    clip = jnp.minimum(1.0, CLIP / (norm[0:1, 0:1] + 1e-06))
    columns = w_ada.shape[0]
    rounded = conds[...].astype(BF).astype(F32)
    turned_mod = dmod[...].T
    g_ada = turned_mod[0:columns, 0:1] * rounded[0:1, :]
    for k in range(1, 4):
        g_ada += turned_mod[0:columns, k : k + 1] * rounded[k : k + 1, :]
    narrow = moments[0].shape[1]
    grads = (
        g_vec[0:9, 0:narrow],
        g_ada,
        g_qkv[...],
        g_attn[...],
        g_in[...],
        g_out[...],
    )
    weights = (
        own_vec[0:9, 0:narrow],
        w_ada[...],
        w_qkv[...],
        w_attn[...],
        w_in[...],
        w_out[...],
    )
    for k in range(6):
        results = adam_step(
            weights[k],
            grads[k] * clip,
            moments[2 * k][...],
            moments[2 * k + 1][...],
            RATE if k else RATE_VECTORS,
            DECAY if k else 0.0,
        )
        for n in range(3):
            outs[3 + 3 * k + n][...] = results[n]


def run_finish(partial_results, weights, moments):
    shapes = [((1, ROWS, WIDTH), BF), ((1, ROWS, WIDTH), F32), ((1, 1), F32)]
    for moment in moments[::2]:
        shapes += [(moment.shape, F32)] * 3
    whole = pl.BlockSpec(memory_space=pltpu.VMEM)
    specs = [whole] * len(shapes)
    specs[2] = pl.BlockSpec(memory_space=pltpu.SMEM)
    args = (*partial_results, *weights, *moments)
    return pl.pallas_call(
        finish_kernel,
        out_shape=[jax.ShapeDtypeStruct(shape, kind) for shape, kind in shapes],
        in_specs=[whole] * len(args),
        out_specs=specs,
        compiler_params=pltpu.CompilerParams(vmem_limit_bytes=60 * 1024 * 1024),
    )(*args)


def slices(
    tokens_in,
    cotangent,
    timesteps,
    span_start,
    span_len,
    vectors,
    w_ada,
    w_qkv,
    w_attn,
    w_in,
    w_out,
    m_vec,
    v_vec,
    m_ada,
    v_ada,
    m_qkv,
    v_qkv,
    m_attn,
    v_attn,
    m_in,
    v_in,
    m_out,
    v_out,
):
    partial_results = run_layer(
        timesteps,
        span_start,
        span_len,
        tokens_in,
        cotangent,
        vectors,
        w_ada.T,
        w_qkv,
        w_attn,
        w_in,
        w_out,
    )
    moments = (
        m_vec,
        v_vec,
        m_ada.T,
        v_ada.T,
        m_qkv,
        v_qkv,
        m_attn,
        v_attn,
        m_in,
        v_in,
        m_out,
        v_out,
    )
    results = run_finish(partial_results, (w_ada.T, w_qkv, w_attn, w_in, w_out), moments)
    ada_results = [result.T for result in results[6:9]]
    return (*results[:2], results[2].reshape(()), *results[3:6], *ada_results, *results[9:])


def solution(mesh):
    in_specs = (
        P("dp", "seq", None),
        P("dp", "seq", None),
        P("dp"),
        P("dp"),
        P("dp"),
        P(),
        P(None, ("dp", "seq")),
        P(("dp", "seq"), None),
        P(("dp", "seq"), None),
        P(("dp", "seq"), None),
        P(("dp", "seq"), None),
        P(None, ("dp", "seq")),
        P(None, ("dp", "seq")),
        P(None, ("dp", "seq")),
        P(None, ("dp", "seq")),
        P(("dp", "seq"), None),
        P(("dp", "seq"), None),
        P(("dp", "seq"), None),
        P(("dp", "seq"), None),
        P(("dp", "seq"), None),
        P(("dp", "seq"), None),
        P(("dp", "seq"), None),
        P(("dp", "seq"), None),
    )
    out_specs = (
        P("dp", "seq", None),
        P("dp", "seq", None),
        P(),
        P(None, ("dp", "seq")),
        P(None, ("dp", "seq")),
        P(None, ("dp", "seq")),
        P(None, ("dp", "seq")),
        P(None, ("dp", "seq")),
        P(None, ("dp", "seq")),
        P(("dp", "seq"), None),
        P(("dp", "seq"), None),
        P(("dp", "seq"), None),
        P(("dp", "seq"), None),
        P(("dp", "seq"), None),
        P(("dp", "seq"), None),
        P(("dp", "seq"), None),
        P(("dp", "seq"), None),
        P(("dp", "seq"), None),
        P(("dp", "seq"), None),
        P(("dp", "seq"), None),
        P(("dp", "seq"), None),
    )
    sizes = dict(mesh.shape)
    local = slices if (sizes["dp"], sizes["seq"]) == (4, 8) else plain
    return jax.shard_map(local, mesh=mesh, in_specs=in_specs, out_specs=out_specs, check_vma=False)
```

```python
from functools import partial
import math
from types import SimpleNamespace

import jax
import jax.numpy as jnp
from jax import lax
from jax.experimental import pallas as pl
from jax.experimental.pallas import tpu as pltpu
from jax.sharding import PartitionSpec as P

HD = 64
COND = 128
STEP = 10


BETA_ONE = 0.9
BETA_TWO = 0.999
ADAM_EPS = 1e-08
RATE = 0.1
RATE_VECTORS = 0.3
DECAY = 0.01
CLIP = 1.0
NORM_EPS = 1e-05


def cond_input(timesteps):
    half_cond = COND // 2
    freqs = jnp.exp(jnp.arange(half_cond, dtype=jnp.float32) * (-math.log(10000.0) / half_cond))
    angles = timesteps.astype(jnp.float32)[:, None] * freqs[None, :]
    return jax.nn.silu(jnp.concatenate([jnp.cos(angles), jnp.sin(angles)], axis=1))


def rotary_tables(positions):
    half_head = HD // 2
    inverse = jnp.exp(jnp.arange(half_head, dtype=jnp.float32) * (-math.log(10000.0) / half_head))
    angles = positions.astype(jnp.float32)[:, None] * inverse[None, :]
    return (jnp.cos(angles), jnp.sin(angles))


def rotate(values, cosines, sines):
    half_head = values.shape[-1] // 2
    first = values[..., :half_head]
    second = values[..., half_head:]
    cos_b = cosines[:, None, :]
    sin_b = sines[:, None, :]
    return jnp.concatenate(
        [first * cos_b - second * sin_b, second * cos_b + first * sin_b], axis=-1
    )


def rotate_back(grads, cosines, sines):
    half_head = grads.shape[-1] // 2
    first = grads[..., :half_head]
    second = grads[..., half_head:]
    cos_b = cosines[:, None, :]
    sin_b = sines[:, None, :]
    return jnp.concatenate(
        [first * cos_b + second * sin_b, second * cos_b - first * sin_b], axis=-1
    )


def normalize(values):
    centre = jnp.mean(values, axis=-1, keepdims=True)
    centred = values - centre
    inverse = lax.rsqrt(jnp.mean(centred * centred, axis=-1, keepdims=True) + NORM_EPS)
    return (centred * inverse, inverse)


def norm_back(normed, inverse, grad):
    return inverse * (
        grad
        - jnp.mean(grad, axis=-1, keepdims=True)
        - normed * jnp.mean(grad * normed, axis=-1, keepdims=True)
    )


def split_kv(block, width):
    seqs, block_rows = (block.shape[0], block.shape[1])
    keys = block[..., :width].reshape(seqs, block_rows, width // HD, HD)
    values = block[..., width:].reshape(seqs, block_rows, width // HD, HD)
    return (keys, values)


def attend_piece(carry, piece, queries, width, factor):
    piece_rows = piece.shape[1]
    size = math.gcd(piece_rows, 512)

    def attend_one_block(index, state):
        running, denom, accum = state
        block = lax.dynamic_slice_in_dim(piece, index * size, size, 1)
        keys, values = split_kv(block, width)
        scores = (
            jnp.einsum("sqhd,skhd->shqk", queries, keys, preferred_element_type=jnp.float32)
            * factor
        )
        highest = jnp.maximum(running, jnp.max(scores, axis=-1))
        shrink = jnp.exp(running - highest)
        weights = jnp.exp(scores - highest[..., None])
        denom = denom * shrink + jnp.sum(weights, axis=-1)
        accum = accum * shrink[..., None] + jnp.einsum(
            "shqk,skhd->shqd",
            weights.astype(jnp.bfloat16),
            values,
            preferred_element_type=jnp.float32,
        )
        return (highest, denom, accum)

    return lax.fori_loop(0, piece_rows // size, attend_one_block, carry)


def block_grads(block, queries, grad_out, logsum, delta, width, factor):
    keys, values = split_kv(block, width)
    scores = (
        jnp.einsum("sqhd,skhd->shqk", queries, keys, preferred_element_type=jnp.float32) * factor
    )
    probs = jnp.exp(scores - logsum[..., None])
    dprobs = jnp.einsum("sqhd,skhd->shqk", grad_out, values, preferred_element_type=jnp.float32)
    dscores = (probs * (dprobs - delta[..., None])).astype(jnp.bfloat16)
    return (keys, probs, dscores)


def query_grads(kv_all, queries, grad_out, logsum, delta, width, factor):
    total_rows = kv_all.shape[1]
    size = math.gcd(total_rows, 512)

    def query_one_block(index, accum):
        block = lax.dynamic_slice_in_dim(kv_all, index * size, size, 1)
        keys, probs, dscores = block_grads(block, queries, grad_out, logsum, delta, width, factor)
        return accum + factor * jnp.einsum(
            "shqk,skhd->sqhd", dscores, keys, preferred_element_type=jnp.float32
        )

    return lax.fori_loop(
        0, total_rows // size, query_one_block, jnp.zeros(queries.shape, jnp.float32)
    )


def key_grads(kv_all, queries, grad_out, logsum, delta, width, factor, count):
    size = math.gcd(count, 512)
    seqs = queries.shape[0]

    def key_one_block(index, accum):
        block = lax.dynamic_slice_in_dim(kv_all, index * size, size, 1)
        keys, probs, dscores = block_grads(block, queries, grad_out, logsum, delta, width, factor)
        grad_vals = jnp.einsum(
            "shqk,sqhd->skhd",
            probs.astype(jnp.bfloat16),
            grad_out,
            preferred_element_type=jnp.float32,
        )
        grad_keys = factor * jnp.einsum(
            "shqk,sqhd->skhd", dscores, queries, preferred_element_type=jnp.float32
        )
        joined = jnp.concatenate(
            [grad_keys.reshape(seqs, size, width), grad_vals.reshape(seqs, size, width)], axis=-1
        )
        return lax.dynamic_update_slice_in_dim(
            accum, jnp.transpose(joined, (1, 0, 2)), index * size, 0
        )

    initial = jnp.zeros((count, seqs, 2 * width), jnp.float32)
    return lax.fori_loop(0, count // size, key_one_block, initial)


def adam_step(weight, grad, first, second, rate, decay_rate):
    new_first = BETA_ONE * first + (1.0 - BETA_ONE) * grad
    new_second = BETA_TWO * second + (1.0 - BETA_TWO) * grad * grad
    fixed_first = new_first / (1.0 - BETA_ONE**STEP)
    fixed_second = new_second / (1.0 - BETA_TWO**STEP)
    new_weight = weight - rate * (
        fixed_first / (jnp.sqrt(fixed_second) + ADAM_EPS) + decay_rate * weight
    )
    return (new_first, new_second, new_weight)


def mod_back(grad_hidden, ln_values, normed, scale_part, gain):
    grad_shift = jnp.sum(grad_hidden, axis=1)
    grad_scale = jnp.sum(grad_hidden * ln_values, axis=1)
    grad_ln = grad_hidden * (1.0 + scale_part)
    grad_gain = jnp.sum(grad_ln * normed, axis=(0, 1))
    return (grad_shift, grad_scale, grad_gain, grad_ln * gain)


def plain(
    tokens_in,
    cotangent,
    timesteps,
    span_start,
    span_len,
    vectors,
    w_ada,
    w_qkv,
    w_attn,
    w_in,
    w_out,
    m_vec,
    v_vec,
    m_ada,
    v_ada,
    m_qkv,
    v_qkv,
    m_attn,
    v_attn,
    m_in,
    v_in,
    m_out,
    v_out,
):
    seqs, group, width = tokens_in.shape
    heads = width // HD
    factor = HD ** (-0.5)
    flat_rows = seqs * group
    full_ada, full_qkv, full_attn, full_in, full_out = (
        lax.all_gather(w_ada.astype(jnp.bfloat16), ("dp", "seq"), axis=1, tiled=True),
        lax.all_gather(w_qkv.astype(jnp.bfloat16), ("dp", "seq"), axis=0, tiled=True),
        lax.all_gather(w_attn.astype(jnp.bfloat16), ("dp", "seq"), axis=0, tiled=True),
        lax.all_gather(w_in.astype(jnp.bfloat16), ("dp", "seq"), axis=0, tiled=True),
        lax.all_gather(w_out.astype(jnp.bfloat16), ("dp", "seq"), axis=0, tiled=True),
    )
    positions = lax.axis_index("seq") * group + jnp.arange(group, dtype=jnp.int32)
    masked = (positions[None, :] >= span_start[:, None]) & (
        positions[None, :] < (span_start + span_len)[:, None]
    )
    cond_bf = cond_input(timesteps).astype(jnp.bfloat16)
    modulation = jnp.dot(cond_bf, full_ada, preferred_element_type=jnp.float32) + vectors[
        2:8
    ].reshape(1, 6 * width)
    pieces = [modulation[:, which * width : (which + 1) * width][:, None, :] for which in range(6)]
    shift_one, scale_one, gate_one, shift_two, scale_two, gate_two = pieces
    start_tokens = jnp.where(
        masked[..., None], vectors[8][None, None, :], tokens_in.astype(jnp.float32)
    )
    normed_one, inv_one = normalize(start_tokens)
    ln_one = normed_one * vectors[0]
    hidden_one = (
        (ln_one * (1.0 + scale_one) + shift_one).astype(jnp.bfloat16).reshape(flat_rows, width)
    )
    projected = jnp.dot(hidden_one, full_qkv, preferred_element_type=jnp.float32).reshape(
        seqs, group, 3 * width
    )
    cosines, sines = rotary_tables(positions)
    queries = rotate(projected[..., :width].reshape(seqs, group, heads, HD), cosines, sines).astype(
        jnp.bfloat16
    )
    keys_here = rotate(
        projected[..., width : 2 * width].reshape(seqs, group, heads, HD), cosines, sines
    ).astype(jnp.bfloat16)
    values_here = projected[..., 2 * width :].astype(jnp.bfloat16)
    kv_local = jnp.concatenate([keys_here.reshape(seqs, group, width), values_here], axis=-1)
    initial = (
        jnp.full((seqs, heads, group), -1e30, jnp.float32),
        jnp.zeros((seqs, heads, group), jnp.float32),
        jnp.zeros((seqs, heads, group, HD), jnp.float32),
    )
    running, denom, accum = attend_piece(
        initial, lax.all_gather(kv_local, "seq", axis=1, tiled=True), queries, width, factor
    )
    attn_heads = accum / denom[..., None]
    logsum = running + jnp.log(denom)
    attn_rows = jnp.transpose(attn_heads, (0, 2, 1, 3)).reshape(flat_rows, width)
    attn_bf = attn_rows.astype(jnp.bfloat16)
    branch_one = jnp.dot(attn_bf, full_attn, preferred_element_type=jnp.float32).reshape(
        seqs, group, width
    )
    mid_tokens = start_tokens + gate_one * branch_one
    normed_two, inv_two = normalize(mid_tokens)
    ln_two = normed_two * vectors[1]
    hidden_two = (
        (ln_two * (1.0 + scale_two) + shift_two).astype(jnp.bfloat16).reshape(flat_rows, width)
    )
    pre_act = jnp.dot(hidden_two, full_in, preferred_element_type=jnp.float32)
    activ, gelu_back = jax.vjp(partial(jax.nn.gelu, approximate=True), pre_act)
    activ_bf = activ.astype(jnp.bfloat16)
    branch_two = jnp.dot(activ_bf, full_out, preferred_element_type=jnp.float32).reshape(
        seqs, group, width
    )
    block_out = (mid_tokens + gate_two * branch_two).astype(jnp.bfloat16)
    grad_y = cotangent.astype(jnp.float32)
    grad_gate_two = jnp.sum(grad_y * branch_two, axis=1)
    grad_branch_two = (grad_y * gate_two).astype(jnp.bfloat16).reshape(flat_rows, width)
    grad_w_out = jnp.dot(activ_bf.T, grad_branch_two, preferred_element_type=jnp.float32)
    grad_activ = jnp.dot(grad_branch_two, full_out.T, preferred_element_type=jnp.float32)
    grad_pre = gelu_back(grad_activ)[0].astype(jnp.bfloat16)
    grad_w_in = jnp.dot(hidden_two.T, grad_pre, preferred_element_type=jnp.float32)
    grad_hidden_two = jnp.dot(grad_pre, full_in.T, preferred_element_type=jnp.float32).reshape(
        seqs, group, width
    )
    grad_shift_two, grad_scale_two, grad_gain_two, grad_normed_two = mod_back(
        grad_hidden_two, ln_two, normed_two, scale_two, vectors[1]
    )
    grad_mid = grad_y + norm_back(normed_two, inv_two, grad_normed_two)
    grad_gate_one = jnp.sum(grad_mid * branch_one, axis=1)
    grad_branch_one = (grad_mid * gate_one).astype(jnp.bfloat16).reshape(flat_rows, width)
    grad_w_attn = jnp.dot(attn_bf.T, grad_branch_one, preferred_element_type=jnp.float32)
    grad_attn_bf = (
        jnp.dot(grad_branch_one, full_attn.T, preferred_element_type=jnp.float32)
        .astype(jnp.bfloat16)
        .reshape(seqs, group, heads, HD)
    )
    delta = jnp.einsum("sqhd,shqd->shq", grad_attn_bf.astype(jnp.float32), attn_heads)
    kv_all = lax.all_gather(kv_local, "seq", axis=1, tiled=True)
    grad_queries = query_grads(kv_all, queries, grad_attn_bf, logsum, delta, width, factor)
    grad_kv = jnp.transpose(
        lax.psum_scatter(
            key_grads(
                kv_all,
                queries,
                grad_attn_bf,
                logsum,
                delta,
                width,
                factor,
                group * lax.axis_size("seq"),
            ).astype(jnp.bfloat16),
            "seq",
            scatter_dimension=0,
            tiled=True,
        ).astype(jnp.float32),
        (1, 0, 2),
    )
    grad_keys = grad_kv[..., :width].reshape(seqs, group, heads, HD)
    grad_qkv = jnp.concatenate(
        [
            rotate_back(grad_queries, cosines, sines).reshape(seqs, group, width),
            rotate_back(grad_keys, cosines, sines).reshape(seqs, group, width),
            grad_kv[..., width:],
        ],
        axis=-1,
    )
    grad_qkv = grad_qkv.astype(jnp.bfloat16).reshape(flat_rows, 3 * width)
    grad_w_qkv = jnp.dot(hidden_one.T, grad_qkv, preferred_element_type=jnp.float32)
    grad_hidden_one = jnp.dot(grad_qkv, full_qkv.T, preferred_element_type=jnp.float32).reshape(
        seqs, group, width
    )
    grad_shift_one, grad_scale_one, grad_gain_one, grad_normed_one = mod_back(
        grad_hidden_one, ln_one, normed_one, scale_one, vectors[0]
    )
    grad_start = grad_mid + norm_back(normed_one, inv_one, grad_normed_one)
    grad_mask_row = jnp.sum(jnp.where(masked[..., None], grad_start, 0.0), axis=(0, 1))
    grad_input = jnp.where(masked[..., None], 0.0, grad_start)
    grad_mod = jnp.concatenate(
        [
            grad_shift_one,
            grad_scale_one,
            grad_gate_one,
            grad_shift_two,
            grad_scale_two,
            grad_gate_two,
        ],
        axis=1,
    )
    grad_w_ada = jnp.dot(cond_bf.astype(jnp.float32).T, grad_mod, precision=lax.Precision.HIGHEST)
    grad_vectors = jnp.concatenate(
        [
            grad_gain_one[None, :],
            grad_gain_two[None, :],
            jnp.sum(grad_mod, axis=0).reshape(6, width),
            grad_mask_row[None, :],
        ],
        axis=0,
    )
    red_ada, red_qkv, red_attn, red_in, red_out, red_vec = (
        lax.psum_scatter(grad_w_ada, ("dp", "seq"), scatter_dimension=1, tiled=True),
        lax.psum_scatter(grad_w_qkv, ("dp", "seq"), scatter_dimension=0, tiled=True),
        lax.psum_scatter(grad_w_attn, ("dp", "seq"), scatter_dimension=0, tiled=True),
        lax.psum_scatter(grad_w_in, ("dp", "seq"), scatter_dimension=0, tiled=True),
        lax.psum_scatter(grad_w_out, ("dp", "seq"), scatter_dimension=0, tiled=True),
        lax.psum_scatter(grad_vectors, ("dp", "seq"), scatter_dimension=1, tiled=True),
    )
    local_squares = jnp.float32(0.0)
    for reduced in (red_vec, red_ada, red_qkv, red_attn, red_in, red_out):
        local_squares = local_squares + jnp.sum(reduced * reduced)
    grad_norm = jnp.sqrt(lax.psum(local_squares, ("dp", "seq")))
    clip_factor = jnp.minimum(1.0, CLIP / (grad_norm + 1e-06))
    columns = red_vec.shape[1]
    own_vectors = lax.dynamic_slice_in_dim(
        vectors, lax.axis_index(("dp", "seq")) * columns, columns, 1
    )
    vec_out = adam_step(own_vectors, red_vec * clip_factor, m_vec, v_vec, RATE_VECTORS, 0.0)
    ada_out = adam_step(w_ada, red_ada * clip_factor, m_ada, v_ada, RATE, DECAY)
    qkv_out = adam_step(w_qkv, red_qkv * clip_factor, m_qkv, v_qkv, RATE, DECAY)
    attn_out = adam_step(w_attn, red_attn * clip_factor, m_attn, v_attn, RATE, DECAY)
    in_out = adam_step(w_in, red_in * clip_factor, m_in, v_in, RATE, DECAY)
    out_out = adam_step(w_out, red_out * clip_factor, m_out, v_out, RATE, DECAY)
    return (
        block_out,
        grad_input,
        grad_norm,
        vec_out[0],
        vec_out[1],
        vec_out[2],
        ada_out[0],
        ada_out[1],
        ada_out[2],
        qkv_out[0],
        qkv_out[1],
        qkv_out[2],
        attn_out[0],
        attn_out[1],
        attn_out[2],
        in_out[0],
        in_out[1],
        in_out[2],
        out_out[0],
        out_out[1],
        out_out[2],
    )


F32, BF = jnp.float32, jnp.bfloat16
MESH = pl.DeviceIdType.MESH
DP, LINE, SEQ, CHIPS, ALL = 4, 4, 8, 16, 32
ROWS, WIDTH, PACK = 128, 768, 640
HALF = WIDTH // 2
HALVES = ((0, 0), (0, 1), (0, 2), (2, 2), (1, 0), (1, 1), (1, 2), None, (2, 0), (2, 1))

def numbered(**counts):
    at = {}
    for name, count in counts.items():
        at[name] = sum(counts[other] for other in at)
    return SimpleNamespace(**at), sum(counts.values())


S, SEM_COUNT = numbered(
    cond=1,
    mix_qkv=1,
    mix_in=1,
    mix_attn=1,
    mod=1,
    w_qkv=1,
    w_attn=1,
    w_in=1,
    w_out=1,
    group_qkv=1,
    group_attn=1,
    fw_qkv=1,
    fw_attn=1,
    fw_in=1,
    fw_out=1,
    tok=4,
    h2=4,
    dm=4,
    xf=4,
    o=1,
    mm=1,
    dh2=1,
    do=1,
    gp=1,
    dh1=1,
    pair_out=1,
    pair_in=1,
    pair_attn=1,
    pair_qkv=1,
    plane_attn=1,
    plane_qkv=1,
    line_out=1,
    line_in=1,
    line_attn=1,
    line_qkv=1,
    last_in=1,
    last_attn=1,
    last_qkv=1,
    early=1,
    early2=1,
    late=1,
    late2=1,
    sq=1,
)

SCRATCH = dict(
    wide_qkv=((48, 3072), F32),
    wide_in=((48, 3072), F32),
    wide_attn=((48, 768), F32),
    s_qkv=((48, 3072), BF),
    s_in=((48, 3072), BF),
    s_attn=((48, 768), BF),
    s_out=((96, 768), BF),
    w_qkv=((768, 768), BF),
    w_in=((768, 768), BF),
    w_attn=((768, 768), BF),
    w_out=((4, 2, 96, 768), BF),
    conds_all=((4, 8, 128), F32),
    mod_send=((4, 4, 128), F32),
    mod_got=((32, 4, 128), F32),
    mod_flat=((40, 128), F32),
    mod_pad=((8, 384), F32),
    turn=((2, 4, 128, 128), F32),
    dmod_flat=((4, 40, 128), F32),
    mod=((8, 768), F32),
    x0=((128, 768), F32),
    n1=((128, 768), F32),
    inv1=((128, 128), F32),
    x1=((128, 768), F32),
    n2=((128, 768), F32),
    inv2=((128, 128), F32),
    a=((128, 768), F32),
    dx1=((128, 768), F32),
    toks=((4, 128, 768), BF),
    h1=((4, 128, 768), BF),
    h2=((4, 128, 768), BF),
    dm=((4, 128, 768), BF),
    gb=((4, 128, 768), BF),
    du=((4, 128, 768), BF),
    xb=((2, 4, 128, 640), BF),
    pt=((3, 1024, 512), BF),
    ot=((2, 128, 512), F32),
    os=((4, 128, 256), BF),
    ob=((4, 128, 256), BF),
    mms=((4, 128, 768), BF),
    mmr=((4, 128, 768), BF),
    dhs=((4, 128, 768), BF),
    dhr=((4, 128, 768), BF),
    das=((128, 768), BF),
    dos=((4, 128, 256), BF),
    dob=((4, 128, 256), BF),
    dst=((3, 1024, 512), BF),
    ga=((512, 640), F32),
    gps=((512, 512), BF),
    gpr=((512, 512), BF),
    dqkv=((4, 128, 768), BF),
    d1s=((4, 128, 768), BF),
    d1r=((4, 128, 768), BF),
    g_out=((4, 2, 96, 768), BF),
    g_in=((2, 768, 384), BF),
    g_attn=((2, 768, 384), BF),
    g_qkv=((2, 768, 384), BF),
    p_out=((4, 96, 768), BF),
    p_in=((768, 384), BF),
    p_attn=((768, 384), BF),
    p_qkv=((768, 384), BF),
    q_attn=((4, 192, 384), BF),
    q_qkv=((4, 192, 384), BF),
    m_attn=((192, 384), BF),
    m_qkv=((192, 384), BF),
    r_out=((4, 96, 768), BF),
    r_in=((16, 48, 384), BF),
    r_attn=((4, 48, 384), BF),
    r_qkv=((4, 48, 384), BF),
    t_in=((4, 48, 384), F32),
    t_attn=((1, 48, 384), F32),
    t_qkv=((4, 48, 384), F32),
    f_in=((4, 2, 24, 384), F32),
    f_attn=((1, 2, 24, 384), F32),
    f_qkv=((4, 2, 24, 384), F32),
    early=((8, 768), F32),
    early_got=((8, 8, 768), F32),
    early_all=((4, 8, 768), F32),
    late=((4, 768), F32),
    late_got=((8, 4, 768), F32),
    late_all=((4, 4, 768), F32),
    sq=((32, 1, 128), F32),
)


def dot(left, right):
    return jnp.dot(left, right, preferred_element_type=F32)


def dot_nt(left, right):
    return lax.dot_general(left, right, (((1,), (1,)), ((), ())), preferred_element_type=F32)


def dot_tn(left, right):
    return lax.dot_general(left, right, (((0,), (0,)), ((), ())), preferred_element_type=F32)


def loop(count, body, start=0):
    def step(index, carry):
        body(index)
        return carry

    lax.fori_loop(start, count, step, 0)


def layer_kernel(
    i_time,
    i_start,
    i_len,
    i_tok,
    i_cot,
    i_vec,
    i_wada,
    i_wqkv,
    i_wattn,
    i_win,
    i_wout,
    o_y,
    o_dx,
    o_norm,
    o_gqkv,
    o_gattn,
    o_gin,
    o_gout,
    o_dmod,
    o_gvec,
    o_vec,
    o_conds,
    *scratch,
):
    r = SimpleNamespace(**dict(zip(SCRATCH, scratch)))
    send_sems, recv_sems = scratch[-2:]
    b, s = lax.axis_index("dp"), lax.axis_index("seq")
    z, c = lax.div(s, 2), lax.rem(s, 2)
    mate = s + 1 - 2 * c
    chip = b * LINE + z
    me = b * SEQ + s
    drains = []

    def push(src, dst, at, to_b, to_s):
        pltpu.make_async_remote_copy(
            src_ref=src,
            dst_ref=dst,
            send_sem=send_sems.at[at],
            recv_sem=recv_sems.at[at],
            device_id=(to_b, to_s),
            device_id_type=MESH,
        ).start()

    def keep(src, dst, at):
        pltpu.make_async_copy(src, dst, recv_sems.at[at]).start()

    def got(at, like):
        pltpu.make_async_copy(like, like, recv_sems.at[at]).wait()

    def left(at, like):
        pltpu.make_async_copy(like, like, send_sems.at[at]).wait()

    def sent(at, like):
        drains.append((at, like))

    near = (b, b + 1 - 2 * lax.rem(b, 2), b + 2 - 4 * lax.div(b, 2), 3 - b)

    def peers(body):
        for k in (1, 2, 3):
            body(k, near[k])

    def stack(body):
        for k in (1, 2, 3):
            body(lax.rem(z + k, LINE))

    lane = lax.broadcasted_iota(jnp.int32, (1, 128), 1)
    low = lane < 64
    own24 = pl.ds(pl.multiple_of(24 * c, 8), 24)
    mate24 = pl.ds(pl.multiple_of(24 * (1 - c), 8), 24)
    part = pl.ds(pl.multiple_of(HALF * c, 128), HALF)
    chip_rows = pl.ds(pl.multiple_of(48 * chip, 16), 48)
    group_rows = pl.ds(pl.multiple_of(192 * b, 16), 192)

    barrier = pltpu.get_barrier_semaphore()

    def greet(k):
        other = lax.rem(me + k, ALL)
        pl.semaphore_signal(
            barrier, inc=1, device_id=(lax.div(other, SEQ), lax.rem(other, SEQ)), device_id_type=MESH
        )

    loop(ALL, greet, 1)

    def natural(kind, p, head):
        return kind * WIDTH + 192 * p + 64 * head

    def half_at(ref, column, high):
        tile = ref[:, column // 128 * 128 : column // 128 * 128 + 128]
        return tile if (column % 128 == 64) == high else pltpu.roll(tile, 64, 1)

    for p in range(4):
        for tile in range(5):
            pair = []
            for high in (0, 1):
                which = HALVES[2 * tile + high]
                pair.append(
                    jnp.zeros((24, 128), F32)
                    if which is None
                    else half_at(i_wqkv, natural(which[0], p, which[1]), bool(high))
                )
            r.wide_qkv[own24, 768 * p + 128 * tile : 768 * p + 128 * tile + 128] = jnp.where(
                low, pair[0], pair[1]
            )
        r.wide_qkv[own24, 768 * p + 640 : 768 * p + 768] = jnp.zeros((24, 128), F32)
    r.wide_in[own24, :] = i_win[...]
    r.wide_attn[own24, :] = i_wattn[...]
    r.s_out[...] = i_wout[...].astype(BF)
    lanes8 = lax.broadcasted_iota(jnp.int32, (8, 128), 1)
    half_cond = COND // 2
    speed = jnp.exp((lanes8 % half_cond).astype(F32) * (-math.log(10000.0) / half_cond))
    angle = i_time[0].astype(F32) * speed
    wave = jnp.where(lanes8 < half_cond, jnp.cos(angle), jnp.sin(angle))
    r.conds_all[b] = wave * (1.0 / (1.0 + jnp.exp(-wave)))
    pl.semaphore_wait(barrier, ALL - 1)

    def stack_rows(to):
        push(r.s_out, r.w_out.at[z, c], S.w_out, b, 2 * to + c)

    peers(lambda k, to: push(r.conds_all.at[b], r.conds_all.at[b], S.cond, to, s))
    sent(S.cond, r.conds_all.at[0:3])
    push(r.wide_qkv.at[own24], r.wide_qkv.at[own24], S.mix_qkv, b, mate)
    sent(S.mix_qkv, r.wide_qkv.at[0:24])
    push(r.wide_attn.at[own24], r.wide_attn.at[own24], S.mix_attn, b, mate)
    sent(S.mix_attn, r.wide_attn.at[0:24])
    push(r.wide_in.at[own24], r.wide_in.at[own24], S.mix_in, b, mate)
    sent(S.mix_in, r.wide_in.at[0:24])

    got(S.cond, r.conds_all.at[0:3])
    row8 = lax.broadcasted_iota(jnp.int32, (8, 128), 0)
    cond4 = jnp.zeros((8, 128), F32)
    for k in range(4):
        cond4 = jnp.where(row8 == k, r.conds_all[k], cond4)
    o_conds[...] = cond4
    wide = i_wada.shape[0]
    r.mod_pad[...] = jnp.zeros((8, 384), F32)
    r.mod_pad[:, 0:wide] = dot_nt(cond4.astype(BF), i_wada[...].astype(BF))
    columns = pltpu.roll(r.mod_pad[...], lax.rem(wide * me, 128), 1)
    for k in range(4):
        for t in range(3):
            r.mod_send[k, t : t + 1, :] = columns[k : k + 1, 128 * t : 128 * t + 128]
        r.mod_send[k, 3:4, :] = jnp.zeros((1, 128), F32)

    def send_mod(k):
        other = lax.rem(me + k, ALL)
        ob = lax.div(other, SEQ)
        push(r.mod_send.at[ob], r.mod_got.at[me], S.mod, ob, lax.rem(other, SEQ))

    loop(ALL, send_mod, 1)
    sent(S.mod, r.mod_got.at[0:31])
    keep(r.mod_send.at[b], r.mod_got.at[me], S.mod)

    def block(src, first):
        return src.at[:, pl.ds(pl.multiple_of(first, 128), HALF)]

    def spread(src, dst, at):
        def one(k):
            to = lax.rem(chip + k, CHIPS)
            to_b, to_z = lax.div(to, LINE), lax.rem(to, LINE)
            push(
                block(src, WIDTH * to_b + HALF * c),
                dst.at[chip_rows, part],
                at,
                to_b,
                2 * to_z + c,
            )

        loop(CHIPS, one, 1)
        keep(block(src, WIDTH * b + HALF * c), dst.at[chip_rows, part], at)
        sent(at, dst.at[0:720, 0:HALF])

    def along_line(src, dst, at, step):
        stack(
            lambda to: push(
                block(src, step * to + HALF * c), dst.at[chip_rows, part], at, b, 2 * to + c
            )
        )
        keep(block(src, step * z + HALF * c), dst.at[chip_rows, part], at)
        sent(at, dst.at[0:144, 0:HALF])

    def over_plane(dst, first, at):
        got(first, dst.at[0:192, 0:HALF])
        peers(
            lambda k, to: push(dst.at[group_rows, part], dst.at[group_rows, part], at, to, s)
        )
        sent(at, dst.at[0:576, 0:HALF])

    def share(dst, at, onward, rows):
        got(at, dst.at[0:rows, 0:HALF])
        push(dst.at[:, part], dst.at[:, part], onward, b, mate)
        sent(onward, dst.at[:, 0:HALF])

    got(S.mix_qkv, r.wide_qkv.at[0:24])
    r.s_qkv[...] = r.wide_qkv[...].astype(BF)
    along_line(r.s_qkv, r.w_qkv, S.w_qkv, WIDTH)
    stack(lambda to: push(i_tok.at[0], r.toks.at[z], S.tok + z, b, 2 * to + c))
    sent(S.tok + z, r.toks.at[0:3])
    got(S.mix_attn, r.wide_attn.at[0:24])
    r.s_attn[...] = r.wide_attn[...].astype(BF)
    along_line(r.s_attn, r.w_attn, S.w_attn, 0)

    def start_tokens(tokens, k):
        place = (2 * k + c) * ROWS + lax.broadcasted_iota(jnp.int32, (ROWS, 1), 0)
        hidden = (place >= i_start[0]) & (place < i_start[0] + i_len[0])
        return jnp.where(hidden, i_vec[8:9, :], tokens.astype(F32)), hidden

    x0, _ = start_tokens(i_tok[0], z)
    r.x0[...] = x0
    n1, inv1 = normalize(x0)
    r.n1[...] = n1
    r.inv1[...] = jnp.broadcast_to(inv1, (ROWS, 128))

    got(S.mod, r.mod_got)
    r.mod_flat[...] = jnp.zeros((40, 128), F32)
    for k in range(ALL):
        first = 9 * k // 8
        r.mod_flat[first : first + 3, :] += r.mod_got[k, 0:3, :]
    for k in range(6):
        row = jnp.concatenate(
            [r.mod_flat[6 * k + t : 6 * k + t + 1, :] for t in range(6)], axis=1
        )
        r.mod[k : k + 1, :] = row + i_vec[2 + k : 3 + k, :]

    def mod(k):
        return r.mod[k : k + 1, :]

    def vec(k):
        return i_vec[k : k + 1, :]

    r.h1[z] = (r.n1[...] * vec(0) * (1.0 + mod(1)) + mod(0)).astype(BF)
    r.dm[0] = (i_cot[0].astype(F32) * mod(5)).astype(BF)
    over_plane(r.w_qkv, S.w_qkv, S.group_qkv)
    peers(lambda k, to: push(r.dm.at[0], r.dm.at[k], S.dm + k, to, s))
    for k in (1, 2, 3):
        sent(S.dm + k, r.dm.at[0])

    lanes = lax.broadcasted_iota(jnp.int32, (ROWS, 128), 1)
    first_half = lanes % HD < HD // 2
    speed = jnp.exp((lanes % (HD // 2)).astype(F32) * (-math.log(10000.0) / (HD // 2)))
    row = lax.broadcasted_iota(jnp.int32, (ROWS, 128), 0)

    def table(k):
        angle = ((2 * k + c) * ROWS + row).astype(F32) * speed
        r.turn[0, k] = jnp.cos(angle)
        sine = jnp.sin(angle)
        r.turn[1, k] = jnp.where(first_half, -sine, sine)

    loop(LINE, table)

    got(S.mix_in, r.wide_in.at[0:24])
    r.s_in[...] = r.wide_in[...].astype(BF)

    share(r.w_qkv, S.group_qkv, S.fw_qkv, 576)
    over_plane(r.w_attn, S.w_attn, S.group_attn)
    got(S.fw_qkv, r.w_qkv.at[:, 0:HALF])

    def turned(tile, sign, k):
        other = jnp.where(first_half, pltpu.roll(tile, 96, 1), pltpu.roll(tile, 32, 1))
        return tile * r.turn[0, k] + sign * (other * r.turn[1, k])

    def project(j):
        k = lax.rem(z + j, LINE)

        @pl.when(j > 0)
        def _():
            got(S.tok + k, r.toks.at[0])
            other, _ = start_tokens(r.toks[k], k)
            other, _ = normalize(other)
            r.h1[k] = (other * vec(0) * (1.0 + mod(1)) + mod(0)).astype(BF)

        x = dot(r.h1[k], r.w_qkv[:, 0:PACK])
        tiles = [x[:, 128 * t : 128 * t + 128] for t in range(5)]
        tiles[0] = turned(tiles[0], 1.0, k) * 0.125
        tiles[1] = jnp.where(low, turned(tiles[1], 1.0, k) * 0.125, tiles[1])
        tiles[2] = turned(tiles[2], 1.0, k)
        tiles[3] = turned(tiles[3], 1.0, k)
        for t in range(5):
            r.xb[0, k, :, 128 * t : 128 * t + 128] = tiles[t].astype(BF)
        push(r.xb.at[0, k], r.xb.at[1, k], S.xf + k, b, mate)

    loop(4, project)
    for k in range(4):
        sent(S.xf + k, r.xb.at[0, 0])

    spread(r.s_in, r.w_in, S.w_in)
    for k in range(4):
        got(S.xf + k, r.xb.at[0, 0])

    def tile_of(t):
        return r.xb[:, :, :, 128 * t : 128 * t + 128].reshape(1024, 128)

    heads = ((0, 2, 4, True, True), (0, 2, 4, False, False), (1, 3, 1, True, False))

    def queries(head, first, size):
        q_tile, _, _, q_low, _ = heads[head]
        q = r.xb[0, first : first + size, :, 128 * q_tile : 128 * q_tile + 128]
        return jnp.where(low if q_low else ~low, q.reshape(size * 128, 128), jnp.zeros((), BF))

    for half in range(2):
        at = slice(256 * half, 256 * half + 256)
        for head in range(3):
            scores = dot_nt(tile_of(heads[head][1]), queries(head, 2 * half, 2))
            weights = jnp.exp(scores - jnp.max(scores, axis=0, keepdims=True))
            weights = weights * (1.0 / jnp.sum(weights, axis=0, keepdims=True))
            weights = weights.astype(BF)
            r.pt[head, :, at] = weights
            out = dot_tn(tile_of(heads[head][2]), weights)
            if head == 0:
                r.ot[0, 0:64, at] = out[0:64]
            elif head == 1:
                r.ot[0, 64:128, at] = out[64:128]
            else:
                r.ot[1, 0:64, at] = out[64:128]
                r.ot[1, 64:128, at] = jnp.zeros((64, 256), F32)
        for t in range(2):
            r.os[2 * half : 2 * half + 2, :, 128 * t : 128 * t + 128] = (
                r.ot[t, :, at].T.astype(BF).reshape(2, 128, 128)
            )
        for to in (2 * half, 2 * half + 1):

            @pl.when(z == to)
            def _():
                keep(r.os.at[to], r.ob.at[z], S.o)

            @pl.when(z != to)
            def _():
                push(r.os.at[to], r.ob.at[z], S.o, b, 2 * to + c)

    sent(S.o, r.os.at[0:3])
    stack(stack_rows)
    keep(r.s_out, r.w_out.at[z, c], S.w_out)
    sent(S.w_out, r.w_out.at[0:3, 0])
    share(r.w_attn, S.group_attn, S.fw_attn, 576)
    got(S.fw_attn, r.w_attn.at[:, 0:HALF])
    got(S.o, r.ob)
    a = jnp.zeros((ROWS, WIDTH), F32)
    for p in range(4):
        a += dot(r.ob[p, :, 0:128], r.w_attn[192 * p : 192 * p + 128, :])
        a += dot(r.ob[p, :, 128:192], r.w_attn[192 * p + 128 : 192 * p + 192, :])
    r.a[...] = a
    x1 = r.x0[...] + mod(2) * a
    r.x1[...] = x1
    n2, inv2 = normalize(x1)
    r.n2[...] = n2
    r.inv2[...] = jnp.broadcast_to(inv2, (ROWS, 128))
    r.h2[0] = (n2 * vec(1) * (1.0 + mod(4)) + mod(3)).astype(BF)
    peers(lambda k, to: push(r.h2.at[0], r.h2.at[k], S.h2 + k, to, s))
    for k in (1, 2, 3):
        sent(S.h2 + k, r.h2.at[0])
    got(S.w_out, r.w_out.at[:, 0])
    push(r.w_out.at[:, c], r.w_out.at[:, c], S.fw_out, b, mate)
    sent(S.fw_out, r.w_out.at[:, 0])
    share(r.w_in, S.w_in, S.fw_in, 768)
    got(S.fw_out, r.w_out.at[:, 0])
    got(S.fw_in, r.w_in.at[:, 0:HALF])

    def feed(first, count):
        at = slice(first, first + count)
        size = count * ROWS
        u = dot(r.h2[at].reshape(size, WIDTH), r.w_in[...])
        slope = 0.7978845608028654
        cube = 0.044715
        t = jnp.tanh(slope * (u + cube * u * u * u))
        r.gb[at] = (0.5 * u * (1.0 + t)).astype(BF).reshape(count, ROWS, WIDTH)
        bend = 0.5 * (1.0 + t) + 0.5 * u * (1.0 - t * t) * (slope * (1.0 + 3.0 * cube * u * u))
        back = dot_nt(r.dm[at].reshape(size, WIDTH), r.w_out[...].reshape(WIDTH, WIDTH))
        du = (back * bend).astype(BF)
        r.du[at] = du.reshape(count, ROWS, WIDTH)
        r.dhs[at] = dot_nt(du, r.w_in[...]).astype(BF).reshape(count, ROWS, WIDTH)

    feed(0, 1)
    for first, count in ((1, 2), (3, 1)):
        for k in range(first, first + count):
            got(S.h2 + k, r.h2.at[0])
            got(S.dm + k, r.dm.at[0])
        feed(first, count)
        for k in range(first, first + count):
            push(r.dhs.at[k], r.dhr.at[k], S.dh2, near[k], s)
    sent(S.dh2, r.dhs.at[0:3])
    for t in range(3):
        at = slice(256 * t, 256 * t + 256)
        mm = dot(r.gb[...].reshape(512, WIDTH), r.w_out[:, :, :, at].reshape(WIDTH, 256))
        r.mms[:, :, at] = mm.astype(BF).reshape(4, ROWS, 256)
    peers(lambda k, to: push(r.mms.at[k], r.mmr.at[k], S.mm, to, s))
    sent(S.mm, r.mms.at[0:3])

    def gather(own, others):
        total = own[0].astype(F32)
        for k in (1, 2, 3):
            total += others[k].astype(F32)
        return total

    for k in range(2):
        rows = slice(384 * k, 384 * k + 384)
        result = dot_tn(r.gb[:, :, rows].reshape(512, 384), r.dm[...].reshape(512, 768))
        r.g_out[2 * k : 2 * k + 2] = result.astype(BF).reshape(2, 2, 96, 768)
    push(r.g_out.at[:, 1 - c], r.p_out, S.pair_out, b, mate)
    sent(S.pair_out, r.p_out)

    def outer(left, right, dst):
        for k in range(2):
            rows = slice(384 * k, 384 * k + 384)
            result = dot_tn(
                left[:, :, rows].reshape(512, 384), right[...].reshape(512, 768)
            ).astype(BF)
            dst[0, rows, :] = result[:, 0:HALF]
            dst[1, rows, :] = result[:, HALF:WIDTH]

    def to_mate(grad, dst, at):
        push(grad.at[1 - c], dst, at, b, mate)
        sent(at, dst)

    def pair_sum(grad, pair, at):
        got(at, pair)
        grad[c] = (grad[c].astype(F32) + pair[...].astype(F32)).astype(BF)

    def plane_sum(grad, dst, at):
        def rows(to):
            return grad.at[c, pl.ds(pl.multiple_of(192 * to, 16), 192)]

        peers(lambda k, to: push(rows(to), dst.at[k], at, to, s))
        keep(rows(b), dst.at[0], at)
        sent(at, dst.at[0:3])

    def line_sum(src, total, dst, first, at):
        got(first, src)
        total[...] = (
            (src[0].astype(F32) + src[1].astype(F32)) + (src[2].astype(F32) + src[3].astype(F32))
        ).astype(BF)

        def rows(to):
            return total.at[pl.ds(pl.multiple_of(48 * to, 16), 48)]

        stack(lambda to: push(rows(to), dst.at[z], at, b, 2 * to + c))
        keep(rows(z), dst.at[z], at)
        sent(at, dst.at[0:3])

    def trade(total, final, at):
        push(total.at[:, mate24], final.at[:, c], at, b, mate)
        sent(at, final.at[:, 0])
        final[:, c] = total[:, own24, :]

    outer(r.h2, r.du, r.g_in)
    to_mate(r.g_in, r.p_in, S.pair_in)

    got(S.pair_out, r.p_out)
    for k in range(4):
        r.g_out[k, c] = (r.g_out[k, c].astype(F32) + r.p_out[k].astype(F32)).astype(BF)

    def send_gout(to):
        push(r.g_out.at[to, c], r.r_out.at[z], S.line_out, b, 2 * to + c)

    stack(send_gout)
    keep(r.g_out.at[z, c], r.r_out.at[z], S.line_out)
    sent(S.line_out, r.r_out.at[0:3])

    got(S.dh2, r.dhr.at[0:3])
    dh = gather(r.dhs, r.dhr)
    n2 = r.n2[...]
    inv2 = r.inv2[:, 0:1]
    r.early[...] = jnp.zeros((8, 768), F32)
    r.early[2:3, :] = jnp.sum(dh, axis=0, keepdims=True)
    both = jnp.sum(dh * n2, axis=0, keepdims=True)
    r.early[3:4, :] = both * vec(1)
    r.early[0:1, :] = both * (1.0 + mod(4))
    grad = dh * ((1.0 + mod(4)) * vec(1))
    dx1 = i_cot[0].astype(F32) + norm_back(n2, inv2, grad)
    r.dx1[...] = dx1
    r.early[1:2, :] = jnp.sum(dx1 * r.a[...], axis=0, keepdims=True)
    r.das[...] = (dx1 * mod(2)).astype(BF)
    for p in range(4):
        first = 192 * p
        r.dos[p, :, 0:128] = dot_nt(r.das[...], r.w_attn[first : first + 128, :]).astype(BF)
        tail = dot_nt(r.das[...], r.w_attn[first + 128 : first + 192, :])
        r.dos[p, :, 128:256] = jnp.concatenate(
            [tail, jnp.zeros((ROWS, 64), F32)], axis=1
        ).astype(BF)

    stack(lambda to: push(r.dos.at[to], r.dob.at[z], S.do, b, 2 * to + c))
    keep(r.dos.at[z], r.dob.at[z], S.do)
    sent(S.do, r.dos.at[0:3])

    for p in range(4):
        rows = slice(192 * p, 192 * p + 192)
        result = dot_tn(r.ob[p], r.das[...])[0:192].astype(BF)
        r.g_attn[0, rows, :] = result[:, 0:HALF]
        r.g_attn[1, rows, :] = result[:, HALF:WIDTH]
    to_mate(r.g_attn, r.p_attn, S.pair_attn)

    got(S.mm, r.mmr.at[0:3])
    mm = gather(r.mms, r.mmr)
    o_y[...] = (r.x1[...] + mod(5) * mm).astype(BF)
    r.early[4:5, :] = jnp.sum(i_cot[0].astype(F32) * mm, axis=0, keepdims=True)

    def over_line(src, dst, name):
        def one(k):
            push(src, dst.at[s], name, b, lax.rem(s + k, SEQ))

        loop(SEQ, one, 1)
        keep(src, dst.at[s], name)
        sent(name, dst.at[0:7])

    def over_group(got_ref, dst, name):
        total = got_ref[0]
        for k in range(1, SEQ):
            total += got_ref[k]
        dst[b] = total
        peers(lambda k, to: push(dst.at[b], dst.at[b], name, to, s))
        sent(name, dst.at[0:3])

    over_line(r.early, r.early_got, S.early)

    pair_sum(r.g_in, r.p_in, S.pair_in)

    def send_gin(k):
        to = lax.rem(chip + k, CHIPS)
        push(
            r.g_in.at[c, pl.ds(pl.multiple_of(48 * to, 16), 48)],
            r.r_in.at[chip],
            S.line_in,
            lax.div(to, LINE),
            2 * lax.rem(to, LINE) + c,
        )

    loop(CHIPS, send_gin, 1)
    keep(r.g_in.at[c, chip_rows], r.r_in.at[chip], S.line_in)
    sent(S.line_in, r.r_in.at[0:15])
    pair_sum(r.g_attn, r.p_attn, S.pair_attn)
    plane_sum(r.g_attn, r.q_attn, S.plane_attn)

    got(S.do, r.dob)
    dot0, dot1 = r.dob[:, :, 0:128].reshape(512, 128), r.dob[:, :, 128:256].reshape(512, 128)
    zero = jnp.zeros((), BF)
    moved = pltpu.roll(dot1.astype(F32), 64, 1).astype(BF)
    grads = (jnp.where(low, dot0, zero), jnp.where(low, zero, dot0), moved)
    product = dot0.astype(F32).T * r.ot[0]
    deltas = (
        jnp.sum(product[0:64], axis=0, keepdims=True),
        jnp.sum(product[64:128], axis=0, keepdims=True),
        jnp.sum(dot1.astype(F32).T * r.ot[1], axis=0, keepdims=True),
    )
    for head in range(3):
        values = tile_of(heads[head][2])
        for half in range(2):
            at = slice(256 * half, 256 * half + 256)
            dp = dot_nt(values, grads[head][at])
            r.dst[head, :, at] = (
                r.pt[head, :, at].astype(F32) * (dp - deltas[head][:, at])
            ).astype(BF)

    def key_grads(rows):
        dk = [dot(r.dst[head, rows, :], queries(head, 0, 4)) for head in range(3)]
        dv = [dot(r.pt[head, rows, :], grads[head]) for head in range(3)]
        return (dv[2], dk[0] + dk[1], dk[2], dv[0] + dv[1])

    for t, tile in enumerate(key_grads(slice(512, 1024))):
        r.gps[:, 128 * t : 128 * t + 128] = tile.astype(BF)
    push(r.gps, r.gpr, S.gp, b, mate)
    sent(S.gp, r.gps)
    for t, tile in enumerate(key_grads(slice(0, 512))):
        r.ga[:, 128 * t + 128 : 128 * t + 256] = tile
    for half in range(2):
        at = slice(256 * half, 256 * half + 256)
        turned_q = [dot_tn(tile_of(heads[head][1]), r.dst[head, :, at]) for head in range(3)]
        top = jnp.concatenate([turned_q[0][0:64], turned_q[1][64:128]], axis=0)
        r.ga[at, 0:128] = top.T * 0.125
        r.ga[at, 128:256] += turned_q[2].T * 0.125
    got(S.gp, r.gpr)

    def unproject(j):
        k = lax.rem(z + 1 + j, LINE)
        rows = pl.ds(pl.multiple_of(128 * k, 128), 128)
        tiles = [r.ga[rows, 0:128]] + [
            r.ga[rows, 128 * t : 128 * t + 128]
            + r.gpr[rows, 128 * t - 128 : 128 * t].astype(F32)
            for t in range(1, 5)
        ]
        tiles[0] = turned(tiles[0], -1.0, k)
        tiles[1] = jnp.where(low, turned(tiles[1], -1.0, k), tiles[1])
        tiles[2] = turned(tiles[2], -1.0, k)
        tiles[3] = turned(tiles[3], -1.0, k)
        for t in range(5):
            r.dqkv[k, :, 128 * t : 128 * t + 128] = tiles[t].astype(BF)
        r.dqkv[k, :, PACK:WIDTH] = jnp.zeros((128, 128), BF)
        r.d1s[k] = dot_nt(r.dqkv[k, :, 0:PACK], r.w_qkv[:, 0:PACK]).astype(BF)

        @pl.when(j < 3)
        def _():
            push(r.d1s.at[k], r.d1r.at[z], S.dh1, b, 2 * k + c)

    loop(4, unproject)
    sent(S.dh1, r.d1s.at[0:3])
    outer(r.h1, r.dqkv, r.g_qkv)
    to_mate(r.g_qkv, r.p_qkv, S.pair_qkv)
    line_sum(r.q_attn, r.m_attn, r.r_attn, S.plane_attn, S.line_attn)
    got(S.early, r.early_got)
    over_group(r.early_got, r.early_all, S.early2)
    pair_sum(r.g_qkv, r.p_qkv, S.pair_qkv)
    plane_sum(r.g_qkv, r.q_qkv, S.plane_qkv)

    got(S.line_in, r.r_in)
    for p in range(4):
        r.t_in[p] = (r.r_in[4 * p].astype(F32) + r.r_in[4 * p + 1].astype(F32)) + (
            r.r_in[4 * p + 2].astype(F32) + r.r_in[4 * p + 3].astype(F32)
        )
    trade(r.t_in, r.f_in, S.last_in)
    line_sum(r.q_qkv, r.m_qkv, r.r_qkv, S.plane_qkv, S.line_qkv)

    got(S.dh1, r.d1r.at[0:3])
    dh = r.d1s[z].astype(F32)
    for k in (1, 2, 3):
        dh += r.d1r[lax.rem(z + k, LINE)].astype(F32)
    n1 = r.n1[...]
    both = jnp.sum(dh * n1, axis=0, keepdims=True)
    r.late[0:1, :] = both * (1.0 + mod(1))
    r.late[1:2, :] = jnp.sum(dh, axis=0, keepdims=True)
    r.late[2:3, :] = both * vec(0)
    grad = dh * ((1.0 + mod(1)) * vec(0))
    dx0 = r.dx1[...] + norm_back(n1, r.inv1[:, 0:1], grad)
    _, hidden = start_tokens(i_tok[0], z)
    o_dx[...] = jnp.where(hidden, 0.0, dx0)
    r.late[3:4, :] = jnp.sum(jnp.where(hidden, dx0, 0.0), axis=0, keepdims=True)
    over_line(r.late, r.late_got, S.late)

    got(S.line_out, r.r_out)
    total = (r.r_out[0].astype(F32) + r.r_out[1].astype(F32)) + (
        r.r_out[2].astype(F32) + r.r_out[3].astype(F32)
    )
    o_gout[...] = total
    squares = total * total
    squares = jnp.sum(squares[:, 0:128] + squares[:, 128:256] + squares[:, 256:384]
                      + squares[:, 384:512] + squares[:, 512:640] + squares[:, 640:768],
                      axis=0, keepdims=True)

    def fold(value):
        total = value[:, 0:128] * value[:, 0:128]
        for t in range(1, value.shape[1] // 128):
            total += value[:, 128 * t : 128 * t + 128] * value[:, 128 * t : 128 * t + 128]
        return jnp.sum(total, axis=0, keepdims=True)

    got(S.line_attn, r.r_attn)
    r.t_attn[0] = (r.r_attn[0].astype(F32) + r.r_attn[1].astype(F32)) + (
        r.r_attn[2].astype(F32) + r.r_attn[3].astype(F32)
    )
    trade(r.t_attn, r.f_attn, S.last_attn)
    got(S.line_qkv, r.r_qkv)
    r.t_qkv[...] = r.r_qkv[...].astype(F32)
    trade(r.t_qkv, r.f_qkv, S.last_qkv)
    got(S.late, r.late_got)
    over_group(r.late_got, r.late_all, S.late2)
    got(S.last_in, r.f_in.at[:, 0])
    got(S.last_attn, r.f_attn.at[:, 0])
    for h in range(2):
        for p in range(4):
            value = r.f_in[p, h]
            o_gin[:, 768 * p + 384 * h : 768 * p + 384 * h + 384] = value
            squares += fold(value)
        value = r.f_attn[0, h]
        o_gattn[:, 384 * h : 384 * h + 384] = value
        squares += fold(value)
    got(S.last_qkv, r.f_qkv.at[:, 0])
    where = {which: index for index, which in enumerate(HALVES) if which is not None}

    def packed_half(chunk, high):
        kind, rest = chunk // 12, chunk % 12
        index = where[(kind, rest % 3)]
        t = index // 2
        tile = r.f_qkv[rest // 3, t // 3, :, t % 3 * 128 : t % 3 * 128 + 128]
        return tile if index % 2 == high else pltpu.roll(tile, 64, 1)

    for t in range(18):
        o_gqkv[:, 128 * t : 128 * t + 128] = jnp.where(
            low, packed_half(2 * t, 0), packed_half(2 * t + 1, 1)
        )
    for p in range(4):
        for h in range(2):
            squares += fold(r.f_qkv[p, h])

    r.sq[me] = squares

    def send_sq(k):
        other = lax.rem(me + k, ALL)
        push(r.sq.at[me], r.sq.at[me], S.sq, lax.div(other, SEQ), lax.rem(other, SEQ))

    loop(ALL, send_sq, 1)
    sent(S.sq, r.sq.at[0:31])
    got(S.early2, r.early_all.at[0:3])
    got(S.late2, r.late_all.at[0:3])
    mods = []
    for k in range(4):
        early, late = r.early_all[k], r.late_all[k]
        rows = jnp.concatenate([late[1:3], early[1:5], jnp.zeros((2, 768), F32)], axis=0)
        for n in range(6):
            for m in range(6):
                r.dmod_flat[k, 6 * n + m : 6 * n + m + 1, :] = rows[
                    n : n + 1, 128 * m : 128 * m + 128
                ]
        mods.append(rows)
    gain = jnp.concatenate(
        [
            sum(r.late_all[k][0:1] for k in range(4)),
            sum(r.early_all[k][0:1] for k in range(4)),
            (mods[0] + mods[1] + mods[2] + mods[3])[0:6],
        ],
        axis=0,
    )
    mask_row = sum(r.late_all[k][3:4] for k in range(4))
    gains = jnp.concatenate([gain, mask_row, jnp.zeros((7, 768), F32)], axis=0)
    masters = jnp.concatenate([i_vec[...], jnp.zeros((7, 768), F32)], axis=0)
    own = lax.rem(WIDTH - 24 * me, WIDTH)
    o_gvec[...] = pltpu.roll(gains, own, 1)[:, 0:128]
    o_vec[...] = pltpu.roll(masters, own, 1)[:, 0:128]
    r.mod_pad[...] = jnp.zeros((8, 384), F32)
    window = lax.div(wide * me, 128)
    for k in range(4):
        rows = r.dmod_flat[k, pl.ds(window, 3), :]
        for m in range(3):
            r.mod_pad[k : k + 1, 128 * m : 128 * m + 128] = rows[m : m + 1, :]
    o_dmod[...] = pltpu.roll(r.mod_pad[...], lax.rem(384 - lax.rem(wide * me, 128), 384), 1)[:, 0:256]
    small = jnp.sum(gain * gain) + jnp.sum(mask_row * mask_row)
    conds = [r.conds_all[k][0:1].astype(BF).astype(F32) for k in range(4)]
    for k in range(4):
        for m in range(k, 4):
            term = jnp.sum(mods[k] * mods[m]) * jnp.sum(conds[k] * conds[m])
            small += term if m == k else 2.0 * term
    got(S.sq, r.sq.at[0:31])
    total = r.sq[0]
    for k in range(1, ALL):
        total += r.sq[k]
    o_norm[...] = jnp.broadcast_to(jnp.sqrt(jnp.sum(total) + small), (8, 128))

    for at, like in drains:
        left(at, like)


def run_layer(*args):
    shapes = (
        ((ROWS, WIDTH), BF),
        ((ROWS, WIDTH), F32),
        ((8, 128), F32),
        ((24, 3 * WIDTH), F32),
        ((24, WIDTH), F32),
        ((24, 4 * WIDTH), F32),
        ((96, WIDTH), F32),
        ((8, 256), F32),
        ((16, 128), F32),
        ((16, 128), F32),
        ((8, 128), F32),
    )
    whole = pl.BlockSpec(memory_space=pltpu.VMEM)
    scalar = pl.BlockSpec(memory_space=pltpu.SMEM)
    return pl.pallas_call(
        layer_kernel,
        out_shape=[jax.ShapeDtypeStruct(shape, kind) for shape, kind in shapes],
        in_specs=[scalar] * 3 + [whole] * (len(args) - 3),
        out_specs=[whole] * len(shapes),
        scratch_shapes=[pltpu.VMEM(shape, kind) for shape, kind in SCRATCH.values()]
        + [pltpu.SemaphoreType.DMA((SEM_COUNT,)), pltpu.SemaphoreType.DMA((SEM_COUNT,))],
        compiler_params=pltpu.CompilerParams(
            collective_id=0, has_side_effects=True, vmem_limit_bytes=60 * 1024 * 1024
        ),
    )(*args)


def finish_kernel(
    y, dx, norm, g_qkv, g_attn, g_in, g_out, dmod, g_vec, own_vec, conds, *rest
):
    (w_ada, w_qkv, w_attn, w_in, w_out), moments, outs = rest[:5], rest[5:17], rest[17:]
    outs[0][0] = y[...]
    outs[1][0] = dx[...]
    outs[2][0, 0] = norm[0, 0]
    clip = jnp.minimum(1.0, CLIP / (norm[0:1, 0:1] + 1e-06))
    columns = w_ada.shape[0]
    rounded = conds[...].astype(BF).astype(F32)
    turned_mod = dmod[...].T
    g_ada = turned_mod[0:columns, 0:1] * rounded[0:1, :]
    for k in range(1, 4):
        g_ada += turned_mod[0:columns, k : k + 1] * rounded[k : k + 1, :]
    narrow = moments[0].shape[1]
    grads = (
        g_vec[0:9, 0:narrow],
        g_ada,
        g_qkv[...],
        g_attn[...],
        g_in[...],
        g_out[...],
    )
    weights = (
        own_vec[0:9, 0:narrow],
        w_ada[...],
        w_qkv[...],
        w_attn[...],
        w_in[...],
        w_out[...],
    )
    for k in range(6):
        results = adam_step(
            weights[k],
            grads[k] * clip,
            moments[2 * k][...],
            moments[2 * k + 1][...],
            RATE if k else RATE_VECTORS,
            DECAY if k else 0.0,
        )
        for n in range(3):
            outs[3 + 3 * k + n][...] = results[n]


def run_finish(partial_results, weights, moments):
    shapes = [((1, ROWS, WIDTH), BF), ((1, ROWS, WIDTH), F32), ((1, 1), F32)]
    for moment in moments[::2]:
        shapes += [(moment.shape, F32)] * 3
    whole = pl.BlockSpec(memory_space=pltpu.VMEM)
    specs = [whole] * len(shapes)
    specs[2] = pl.BlockSpec(memory_space=pltpu.SMEM)
    args = (*partial_results, *weights, *moments)
    return pl.pallas_call(
        finish_kernel,
        out_shape=[jax.ShapeDtypeStruct(shape, kind) for shape, kind in shapes],
        in_specs=[whole] * len(args),
        out_specs=specs,
        compiler_params=pltpu.CompilerParams(vmem_limit_bytes=60 * 1024 * 1024),
    )(*args)


def slices(
    tokens_in,
    cotangent,
    timesteps,
    span_start,
    span_len,
    vectors,
    w_ada,
    w_qkv,
    w_attn,
    w_in,
    w_out,
    m_vec,
    v_vec,
    m_ada,
    v_ada,
    m_qkv,
    v_qkv,
    m_attn,
    v_attn,
    m_in,
    v_in,
    m_out,
    v_out,
):
    partial_results = run_layer(
        timesteps,
        span_start,
        span_len,
        tokens_in,
        cotangent,
        vectors,
        w_ada.T,
        w_qkv,
        w_attn,
        w_in,
        w_out,
    )
    moments = (
        m_vec,
        v_vec,
        m_ada.T,
        v_ada.T,
        m_qkv,
        v_qkv,
        m_attn,
        v_attn,
        m_in,
        v_in,
        m_out,
        v_out,
    )
    results = run_finish(partial_results, (w_ada.T, w_qkv, w_attn, w_in, w_out), moments)
    ada_results = [result.T for result in results[6:9]]
    return (*results[:2], results[2].reshape(()), *results[3:6], *ada_results, *results[9:])


def solution(mesh):
    in_specs = (
        P("dp", "seq", None),
        P("dp", "seq", None),
        P("dp"),
        P("dp"),
        P("dp"),
        P(),
        P(None, ("dp", "seq")),
        P(("dp", "seq"), None),
        P(("dp", "seq"), None),
        P(("dp", "seq"), None),
        P(("dp", "seq"), None),
        P(None, ("dp", "seq")),
        P(None, ("dp", "seq")),
        P(None, ("dp", "seq")),
        P(None, ("dp", "seq")),
        P(("dp", "seq"), None),
        P(("dp", "seq"), None),
        P(("dp", "seq"), None),
        P(("dp", "seq"), None),
        P(("dp", "seq"), None),
        P(("dp", "seq"), None),
        P(("dp", "seq"), None),
        P(("dp", "seq"), None),
    )
    out_specs = (
        P("dp", "seq", None),
        P("dp", "seq", None),
        P(),
        P(None, ("dp", "seq")),
        P(None, ("dp", "seq")),
        P(None, ("dp", "seq")),
        P(None, ("dp", "seq")),
        P(None, ("dp", "seq")),
        P(None, ("dp", "seq")),
        P(("dp", "seq"), None),
        P(("dp", "seq"), None),
        P(("dp", "seq"), None),
        P(("dp", "seq"), None),
        P(("dp", "seq"), None),
        P(("dp", "seq"), None),
        P(("dp", "seq"), None),
        P(("dp", "seq"), None),
        P(("dp", "seq"), None),
        P(("dp", "seq"), None),
        P(("dp", "seq"), None),
        P(("dp", "seq"), None),
    )
    sizes = dict(mesh.shape)
    local = slices if (sizes["dp"], sizes["seq"]) == (4, 8) else plain
    return jax.shard_map(local, mesh=mesh, in_specs=in_specs, out_specs=out_specs, check_vma=False)
```

```python
from functools import partial
import math
from types import SimpleNamespace

import jax
import jax.numpy as jnp
from jax import lax
from jax.experimental import pallas as pl
from jax.experimental.pallas import tpu as pltpu
from jax.sharding import PartitionSpec as P

HD = 64
COND = 128
STEP = 10


BETA_ONE = 0.9
BETA_TWO = 0.999
ADAM_EPS = 1e-08
RATE = 0.1
RATE_VECTORS = 0.3
DECAY = 0.01
CLIP = 1.0
NORM_EPS = 1e-05


def cond_input(timesteps):
    half_cond = COND // 2
    freqs = jnp.exp(jnp.arange(half_cond, dtype=jnp.float32) * (-math.log(10000.0) / half_cond))
    angles = timesteps.astype(jnp.float32)[:, None] * freqs[None, :]
    return jax.nn.silu(jnp.concatenate([jnp.cos(angles), jnp.sin(angles)], axis=1))


def rotary_tables(positions):
    half_head = HD // 2
    inverse = jnp.exp(jnp.arange(half_head, dtype=jnp.float32) * (-math.log(10000.0) / half_head))
    angles = positions.astype(jnp.float32)[:, None] * inverse[None, :]
    return (jnp.cos(angles), jnp.sin(angles))


def rotate(values, cosines, sines):
    half_head = values.shape[-1] // 2
    first = values[..., :half_head]
    second = values[..., half_head:]
    cos_b = cosines[:, None, :]
    sin_b = sines[:, None, :]
    return jnp.concatenate(
        [first * cos_b - second * sin_b, second * cos_b + first * sin_b], axis=-1
    )


def rotate_back(grads, cosines, sines):
    half_head = grads.shape[-1] // 2
    first = grads[..., :half_head]
    second = grads[..., half_head:]
    cos_b = cosines[:, None, :]
    sin_b = sines[:, None, :]
    return jnp.concatenate(
        [first * cos_b + second * sin_b, second * cos_b - first * sin_b], axis=-1
    )


def normalize(values):
    centre = jnp.mean(values, axis=-1, keepdims=True)
    centred = values - centre
    inverse = lax.rsqrt(jnp.mean(centred * centred, axis=-1, keepdims=True) + NORM_EPS)
    return (centred * inverse, inverse)


def norm_back(normed, inverse, grad):
    return inverse * (
        grad
        - jnp.mean(grad, axis=-1, keepdims=True)
        - normed * jnp.mean(grad * normed, axis=-1, keepdims=True)
    )


def split_kv(block, width):
    seqs, block_rows = (block.shape[0], block.shape[1])
    keys = block[..., :width].reshape(seqs, block_rows, width // HD, HD)
    values = block[..., width:].reshape(seqs, block_rows, width // HD, HD)
    return (keys, values)


def attend_piece(carry, piece, queries, width, factor):
    piece_rows = piece.shape[1]
    size = math.gcd(piece_rows, 512)

    def attend_one_block(index, state):
        running, denom, accum = state
        block = lax.dynamic_slice_in_dim(piece, index * size, size, 1)
        keys, values = split_kv(block, width)
        scores = (
            jnp.einsum("sqhd,skhd->shqk", queries, keys, preferred_element_type=jnp.float32)
            * factor
        )
        highest = jnp.maximum(running, jnp.max(scores, axis=-1))
        shrink = jnp.exp(running - highest)
        weights = jnp.exp(scores - highest[..., None])
        denom = denom * shrink + jnp.sum(weights, axis=-1)
        accum = accum * shrink[..., None] + jnp.einsum(
            "shqk,skhd->shqd",
            weights.astype(jnp.bfloat16),
            values,
            preferred_element_type=jnp.float32,
        )
        return (highest, denom, accum)

    return lax.fori_loop(0, piece_rows // size, attend_one_block, carry)


def block_grads(block, queries, grad_out, logsum, delta, width, factor):
    keys, values = split_kv(block, width)
    scores = (
        jnp.einsum("sqhd,skhd->shqk", queries, keys, preferred_element_type=jnp.float32) * factor
    )
    probs = jnp.exp(scores - logsum[..., None])
    dprobs = jnp.einsum("sqhd,skhd->shqk", grad_out, values, preferred_element_type=jnp.float32)
    dscores = (probs * (dprobs - delta[..., None])).astype(jnp.bfloat16)
    return (keys, probs, dscores)


def query_grads(kv_all, queries, grad_out, logsum, delta, width, factor):
    total_rows = kv_all.shape[1]
    size = math.gcd(total_rows, 512)

    def query_one_block(index, accum):
        block = lax.dynamic_slice_in_dim(kv_all, index * size, size, 1)
        keys, probs, dscores = block_grads(block, queries, grad_out, logsum, delta, width, factor)
        return accum + factor * jnp.einsum(
            "shqk,skhd->sqhd", dscores, keys, preferred_element_type=jnp.float32
        )

    return lax.fori_loop(
        0, total_rows // size, query_one_block, jnp.zeros(queries.shape, jnp.float32)
    )


def key_grads(kv_all, queries, grad_out, logsum, delta, width, factor, count):
    size = math.gcd(count, 512)
    seqs = queries.shape[0]

    def key_one_block(index, accum):
        block = lax.dynamic_slice_in_dim(kv_all, index * size, size, 1)
        keys, probs, dscores = block_grads(block, queries, grad_out, logsum, delta, width, factor)
        grad_vals = jnp.einsum(
            "shqk,sqhd->skhd",
            probs.astype(jnp.bfloat16),
            grad_out,
            preferred_element_type=jnp.float32,
        )
        grad_keys = factor * jnp.einsum(
            "shqk,sqhd->skhd", dscores, queries, preferred_element_type=jnp.float32
        )
        joined = jnp.concatenate(
            [grad_keys.reshape(seqs, size, width), grad_vals.reshape(seqs, size, width)], axis=-1
        )
        return lax.dynamic_update_slice_in_dim(
            accum, jnp.transpose(joined, (1, 0, 2)), index * size, 0
        )

    initial = jnp.zeros((count, seqs, 2 * width), jnp.float32)
    return lax.fori_loop(0, count // size, key_one_block, initial)


def adam_step(weight, grad, first, second, rate, decay_rate):
    new_first = BETA_ONE * first + (1.0 - BETA_ONE) * grad
    new_second = BETA_TWO * second + (1.0 - BETA_TWO) * grad * grad
    fixed_first = new_first / (1.0 - BETA_ONE**STEP)
    fixed_second = new_second / (1.0 - BETA_TWO**STEP)
    new_weight = weight - rate * (
        fixed_first / (jnp.sqrt(fixed_second) + ADAM_EPS) + decay_rate * weight
    )
    return (new_first, new_second, new_weight)


def mod_back(grad_hidden, ln_values, normed, scale_part, gain):
    grad_shift = jnp.sum(grad_hidden, axis=1)
    grad_scale = jnp.sum(grad_hidden * ln_values, axis=1)
    grad_ln = grad_hidden * (1.0 + scale_part)
    grad_gain = jnp.sum(grad_ln * normed, axis=(0, 1))
    return (grad_shift, grad_scale, grad_gain, grad_ln * gain)


def plain(
    tokens_in,
    cotangent,
    timesteps,
    span_start,
    span_len,
    vectors,
    w_ada,
    w_qkv,
    w_attn,
    w_in,
    w_out,
    m_vec,
    v_vec,
    m_ada,
    v_ada,
    m_qkv,
    v_qkv,
    m_attn,
    v_attn,
    m_in,
    v_in,
    m_out,
    v_out,
):
    seqs, group, width = tokens_in.shape
    heads = width // HD
    factor = HD ** (-0.5)
    flat_rows = seqs * group
    full_ada, full_qkv, full_attn, full_in, full_out = (
        lax.all_gather(w_ada.astype(jnp.bfloat16), ("dp", "seq"), axis=1, tiled=True),
        lax.all_gather(w_qkv.astype(jnp.bfloat16), ("dp", "seq"), axis=0, tiled=True),
        lax.all_gather(w_attn.astype(jnp.bfloat16), ("dp", "seq"), axis=0, tiled=True),
        lax.all_gather(w_in.astype(jnp.bfloat16), ("dp", "seq"), axis=0, tiled=True),
        lax.all_gather(w_out.astype(jnp.bfloat16), ("dp", "seq"), axis=0, tiled=True),
    )
    positions = lax.axis_index("seq") * group + jnp.arange(group, dtype=jnp.int32)
    masked = (positions[None, :] >= span_start[:, None]) & (
        positions[None, :] < (span_start + span_len)[:, None]
    )
    cond_bf = cond_input(timesteps).astype(jnp.bfloat16)
    modulation = jnp.dot(cond_bf, full_ada, preferred_element_type=jnp.float32) + vectors[
        2:8
    ].reshape(1, 6 * width)
    pieces = [modulation[:, which * width : (which + 1) * width][:, None, :] for which in range(6)]
    shift_one, scale_one, gate_one, shift_two, scale_two, gate_two = pieces
    start_tokens = jnp.where(
        masked[..., None], vectors[8][None, None, :], tokens_in.astype(jnp.float32)
    )
    normed_one, inv_one = normalize(start_tokens)
    ln_one = normed_one * vectors[0]
    hidden_one = (
        (ln_one * (1.0 + scale_one) + shift_one).astype(jnp.bfloat16).reshape(flat_rows, width)
    )
    projected = jnp.dot(hidden_one, full_qkv, preferred_element_type=jnp.float32).reshape(
        seqs, group, 3 * width
    )
    cosines, sines = rotary_tables(positions)
    queries = rotate(projected[..., :width].reshape(seqs, group, heads, HD), cosines, sines).astype(
        jnp.bfloat16
    )
    keys_here = rotate(
        projected[..., width : 2 * width].reshape(seqs, group, heads, HD), cosines, sines
    ).astype(jnp.bfloat16)
    values_here = projected[..., 2 * width :].astype(jnp.bfloat16)
    kv_local = jnp.concatenate([keys_here.reshape(seqs, group, width), values_here], axis=-1)
    initial = (
        jnp.full((seqs, heads, group), -1e30, jnp.float32),
        jnp.zeros((seqs, heads, group), jnp.float32),
        jnp.zeros((seqs, heads, group, HD), jnp.float32),
    )
    running, denom, accum = attend_piece(
        initial, lax.all_gather(kv_local, "seq", axis=1, tiled=True), queries, width, factor
    )
    attn_heads = accum / denom[..., None]
    logsum = running + jnp.log(denom)
    attn_rows = jnp.transpose(attn_heads, (0, 2, 1, 3)).reshape(flat_rows, width)
    attn_bf = attn_rows.astype(jnp.bfloat16)
    branch_one = jnp.dot(attn_bf, full_attn, preferred_element_type=jnp.float32).reshape(
        seqs, group, width
    )
    mid_tokens = start_tokens + gate_one * branch_one
    normed_two, inv_two = normalize(mid_tokens)
    ln_two = normed_two * vectors[1]
    hidden_two = (
        (ln_two * (1.0 + scale_two) + shift_two).astype(jnp.bfloat16).reshape(flat_rows, width)
    )
    pre_act = jnp.dot(hidden_two, full_in, preferred_element_type=jnp.float32)
    activ, gelu_back = jax.vjp(partial(jax.nn.gelu, approximate=True), pre_act)
    activ_bf = activ.astype(jnp.bfloat16)
    branch_two = jnp.dot(activ_bf, full_out, preferred_element_type=jnp.float32).reshape(
        seqs, group, width
    )
    block_out = (mid_tokens + gate_two * branch_two).astype(jnp.bfloat16)
    grad_y = cotangent.astype(jnp.float32)
    grad_gate_two = jnp.sum(grad_y * branch_two, axis=1)
    grad_branch_two = (grad_y * gate_two).astype(jnp.bfloat16).reshape(flat_rows, width)
    grad_w_out = jnp.dot(activ_bf.T, grad_branch_two, preferred_element_type=jnp.float32)
    grad_activ = jnp.dot(grad_branch_two, full_out.T, preferred_element_type=jnp.float32)
    grad_pre = gelu_back(grad_activ)[0].astype(jnp.bfloat16)
    grad_w_in = jnp.dot(hidden_two.T, grad_pre, preferred_element_type=jnp.float32)
    grad_hidden_two = jnp.dot(grad_pre, full_in.T, preferred_element_type=jnp.float32).reshape(
        seqs, group, width
    )
    grad_shift_two, grad_scale_two, grad_gain_two, grad_normed_two = mod_back(
        grad_hidden_two, ln_two, normed_two, scale_two, vectors[1]
    )
    grad_mid = grad_y + norm_back(normed_two, inv_two, grad_normed_two)
    grad_gate_one = jnp.sum(grad_mid * branch_one, axis=1)
    grad_branch_one = (grad_mid * gate_one).astype(jnp.bfloat16).reshape(flat_rows, width)
    grad_w_attn = jnp.dot(attn_bf.T, grad_branch_one, preferred_element_type=jnp.float32)
    grad_attn_bf = (
        jnp.dot(grad_branch_one, full_attn.T, preferred_element_type=jnp.float32)
        .astype(jnp.bfloat16)
        .reshape(seqs, group, heads, HD)
    )
    delta = jnp.einsum("sqhd,shqd->shq", grad_attn_bf.astype(jnp.float32), attn_heads)
    kv_all = lax.all_gather(kv_local, "seq", axis=1, tiled=True)
    grad_queries = query_grads(kv_all, queries, grad_attn_bf, logsum, delta, width, factor)
    grad_kv = jnp.transpose(
        lax.psum_scatter(
            key_grads(
                kv_all,
                queries,
                grad_attn_bf,
                logsum,
                delta,
                width,
                factor,
                group * lax.axis_size("seq"),
            ).astype(jnp.bfloat16),
            "seq",
            scatter_dimension=0,
            tiled=True,
        ).astype(jnp.float32),
        (1, 0, 2),
    )
    grad_keys = grad_kv[..., :width].reshape(seqs, group, heads, HD)
    grad_qkv = jnp.concatenate(
        [
            rotate_back(grad_queries, cosines, sines).reshape(seqs, group, width),
            rotate_back(grad_keys, cosines, sines).reshape(seqs, group, width),
            grad_kv[..., width:],
        ],
        axis=-1,
    )
    grad_qkv = grad_qkv.astype(jnp.bfloat16).reshape(flat_rows, 3 * width)
    grad_w_qkv = jnp.dot(hidden_one.T, grad_qkv, preferred_element_type=jnp.float32)
    grad_hidden_one = jnp.dot(grad_qkv, full_qkv.T, preferred_element_type=jnp.float32).reshape(
        seqs, group, width
    )
    grad_shift_one, grad_scale_one, grad_gain_one, grad_normed_one = mod_back(
        grad_hidden_one, ln_one, normed_one, scale_one, vectors[0]
    )
    grad_start = grad_mid + norm_back(normed_one, inv_one, grad_normed_one)
    grad_mask_row = jnp.sum(jnp.where(masked[..., None], grad_start, 0.0), axis=(0, 1))
    grad_input = jnp.where(masked[..., None], 0.0, grad_start)
    grad_mod = jnp.concatenate(
        [
            grad_shift_one,
            grad_scale_one,
            grad_gate_one,
            grad_shift_two,
            grad_scale_two,
            grad_gate_two,
        ],
        axis=1,
    )
    grad_w_ada = jnp.dot(cond_bf.astype(jnp.float32).T, grad_mod, precision=lax.Precision.HIGHEST)
    grad_vectors = jnp.concatenate(
        [
            grad_gain_one[None, :],
            grad_gain_two[None, :],
            jnp.sum(grad_mod, axis=0).reshape(6, width),
            grad_mask_row[None, :],
        ],
        axis=0,
    )
    red_ada, red_qkv, red_attn, red_in, red_out, red_vec = (
        lax.psum_scatter(grad_w_ada, ("dp", "seq"), scatter_dimension=1, tiled=True),
        lax.psum_scatter(grad_w_qkv, ("dp", "seq"), scatter_dimension=0, tiled=True),
        lax.psum_scatter(grad_w_attn, ("dp", "seq"), scatter_dimension=0, tiled=True),
        lax.psum_scatter(grad_w_in, ("dp", "seq"), scatter_dimension=0, tiled=True),
        lax.psum_scatter(grad_w_out, ("dp", "seq"), scatter_dimension=0, tiled=True),
        lax.psum_scatter(grad_vectors, ("dp", "seq"), scatter_dimension=1, tiled=True),
    )
    local_squares = jnp.float32(0.0)
    for reduced in (red_vec, red_ada, red_qkv, red_attn, red_in, red_out):
        local_squares = local_squares + jnp.sum(reduced * reduced)
    grad_norm = jnp.sqrt(lax.psum(local_squares, ("dp", "seq")))
    clip_factor = jnp.minimum(1.0, CLIP / (grad_norm + 1e-06))
    columns = red_vec.shape[1]
    own_vectors = lax.dynamic_slice_in_dim(
        vectors, lax.axis_index(("dp", "seq")) * columns, columns, 1
    )
    vec_out = adam_step(own_vectors, red_vec * clip_factor, m_vec, v_vec, RATE_VECTORS, 0.0)
    ada_out = adam_step(w_ada, red_ada * clip_factor, m_ada, v_ada, RATE, DECAY)
    qkv_out = adam_step(w_qkv, red_qkv * clip_factor, m_qkv, v_qkv, RATE, DECAY)
    attn_out = adam_step(w_attn, red_attn * clip_factor, m_attn, v_attn, RATE, DECAY)
    in_out = adam_step(w_in, red_in * clip_factor, m_in, v_in, RATE, DECAY)
    out_out = adam_step(w_out, red_out * clip_factor, m_out, v_out, RATE, DECAY)
    return (
        block_out,
        grad_input,
        grad_norm,
        vec_out[0],
        vec_out[1],
        vec_out[2],
        ada_out[0],
        ada_out[1],
        ada_out[2],
        qkv_out[0],
        qkv_out[1],
        qkv_out[2],
        attn_out[0],
        attn_out[1],
        attn_out[2],
        in_out[0],
        in_out[1],
        in_out[2],
        out_out[0],
        out_out[1],
        out_out[2],
    )


F32, BF = jnp.float32, jnp.bfloat16
MESH = pl.DeviceIdType.MESH
DP, LINE, SEQ, CHIPS, ALL = 4, 4, 8, 16, 32
ROWS, WIDTH, PACK = 128, 768, 640
HALF = WIDTH // 2
HALVES = ((0, 0), (0, 1), (0, 2), (2, 2), (1, 0), (1, 1), (1, 2), None, (2, 0), (2, 1))

def numbered(**counts):
    at = {}
    for name, count in counts.items():
        at[name] = sum(counts[other] for other in at)
    return SimpleNamespace(**at), sum(counts.values())


S, SEM_COUNT = numbered(
    cond=1,
    mix_qkv=1,
    mix_in=1,
    mix_attn=1,
    mod=1,
    w_qkv=1,
    w_attn=1,
    plane_in=1,
    w_in=4,
    w_out=4,
    group_qkv=1,
    group_attn=1,
    fw_qkv=1,
    fw_attn=1,
    fw_in=1,
    fw_out=1,
    tok=4,
    h2=4,
    dm=4,
    xf=4,
    o=1,
    mm=1,
    dh2=1,
    do=1,
    gp=1,
    dh1=1,
    pair_out=1,
    pair_in=1,
    pair_attn=1,
    pair_qkv=1,
    plane_attn=1,
    plane_qkv=1,
    line_out=1,
    line_in=1,
    line_attn=1,
    line_qkv=1,
    last_in=1,
    last_attn=1,
    last_qkv=1,
    early=1,
    early2=1,
    late=1,
    late2=1,
    sq=1,
)

SCRATCH = dict(
    wide_qkv=((48, 3072), F32),
    wide_in=((48, 3072), F32),
    wide_attn=((48, 768), F32),
    s_qkv=((48, 3072), BF),
    s_in=((48, 3072), BF),
    s_attn=((48, 768), BF),
    w_qkv=((768, 768), BF),
    w_in=((4, 4, 48, 768), BF),
    w_attn=((768, 768), BF),
    w_out=((4, 2, 96, 768), BF),
    conds_all=((4, 8, 128), F32),
    mod_send=((4, 4, 128), F32),
    mod_got=((32, 4, 128), F32),
    mod_flat=((40, 128), F32),
    mod_pad=((8, 384), F32),
    turn=((2, 4, 128, 128), F32),
    dmod_flat=((4, 40, 128), F32),
    mod=((8, 768), F32),
    x0=((128, 768), F32),
    n1=((128, 768), F32),
    inv1=((128, 128), F32),
    x1=((128, 768), F32),
    n2=((128, 768), F32),
    inv2=((128, 128), F32),
    a=((128, 768), F32),
    dx1=((128, 768), F32),
    toks=((4, 128, 768), BF),
    h1=((4, 128, 768), BF),
    h2=((4, 128, 768), BF),
    dm=((4, 128, 768), BF),
    gb=((4, 128, 768), BF),
    du=((4, 128, 768), BF),
    xb=((2, 4, 128, 640), BF),
    pt=((3, 1024, 512), BF),
    ot=((2, 128, 512), F32),
    os=((4, 128, 256), BF),
    ob=((4, 128, 256), BF),
    mms=((4, 128, 768), BF),
    mmr=((4, 128, 768), BF),
    dhs=((4, 128, 768), BF),
    dhr=((4, 128, 768), BF),
    das=((128, 768), BF),
    dos=((4, 128, 256), BF),
    dob=((4, 128, 256), BF),
    dst=((3, 1024, 512), BF),
    ga=((512, 640), F32),
    gps=((512, 512), BF),
    gpr=((512, 512), BF),
    dqkv=((4, 128, 768), BF),
    d1s=((4, 128, 768), BF),
    d1r=((4, 128, 768), BF),
    g_out=((4, 2, 96, 768), BF),
    g_in=((2, 768, 384), BF),
    g_attn=((2, 768, 384), BF),
    g_qkv=((2, 768, 384), BF),
    p_out=((4, 96, 768), BF),
    p_in=((768, 384), BF),
    p_attn=((768, 384), BF),
    p_qkv=((768, 384), BF),
    q_attn=((4, 192, 384), BF),
    q_qkv=((4, 192, 384), BF),
    m_attn=((192, 384), BF),
    m_qkv=((192, 384), BF),
    r_out=((4, 96, 768), BF),
    r_in=((16, 48, 384), BF),
    r_attn=((4, 48, 384), BF),
    r_qkv=((4, 48, 384), BF),
    t_in=((4, 48, 384), F32),
    t_attn=((1, 48, 384), F32),
    t_qkv=((4, 48, 384), F32),
    f_in=((4, 2, 24, 384), F32),
    f_attn=((1, 2, 24, 384), F32),
    f_qkv=((4, 2, 24, 384), F32),
    early=((8, 768), F32),
    early_got=((8, 8, 768), F32),
    early_all=((4, 8, 768), F32),
    late=((4, 768), F32),
    late_got=((8, 4, 768), F32),
    late_all=((4, 4, 768), F32),
    sq=((32, 1, 128), F32),
)


def dot(left, right):
    return jnp.dot(left, right, preferred_element_type=F32)


def dot_nt(left, right):
    return lax.dot_general(left, right, (((1,), (1,)), ((), ())), preferred_element_type=F32)


def dot_tn(left, right):
    return lax.dot_general(left, right, (((0,), (0,)), ((), ())), preferred_element_type=F32)


def loop(count, body, start=0):
    def step(index, carry):
        body(index)
        return carry

    lax.fori_loop(start, count, step, 0)


def layer_kernel(
    i_when,
    i_tok,
    i_cot,
    i_vec,
    i_wada,
    i_wqkv,
    i_wattn,
    i_win,
    i_wout,
    o_y,
    o_dx,
    o_norm,
    o_gqkv,
    o_gattn,
    o_gin,
    o_gout,
    o_dmod,
    o_gvec,
    o_vec,
    o_conds,
    *scratch,
):
    r = SimpleNamespace(**dict(zip(SCRATCH, scratch)))
    send_sems, recv_sems = scratch[-2:]
    b, s = lax.axis_index("dp"), lax.axis_index("seq")
    z, c = lax.div(s, 2), lax.rem(s, 2)
    mate = s + 1 - 2 * c
    chip = b * LINE + z
    me = b * SEQ + s
    drains = []

    def push(src, dst, at, to_b, to_s, out=None):
        pltpu.make_async_remote_copy(
            src_ref=src,
            dst_ref=dst,
            send_sem=send_sems.at[at if out is None else out],
            recv_sem=recv_sems.at[at],
            device_id=(to_b, to_s),
            device_id_type=MESH,
        ).start()

    def keep(src, dst, at):
        pltpu.make_async_copy(src, dst, recv_sems.at[at]).start()

    def got(at, like):
        pltpu.make_async_copy(like, like, recv_sems.at[at]).wait()

    def left(at, like):
        pltpu.make_async_copy(like, like, send_sems.at[at]).wait()

    def sent(at, like):
        drains.append((at, like))

    near = (b, b + 1 - 2 * lax.rem(b, 2), b + 2 - 4 * lax.div(b, 2), 3 - b)

    def peers(body):
        for k in (1, 2, 3):
            body(k, near[k])

    def stack(body):
        for k in (1, 2, 3):
            body(lax.rem(z + k, LINE))

    def line_gather(block, at):
        def one(to):
            @pl.when(jnp.logical_not(((z == 1) & (to == 3)) | ((z == 2) & (to == 0))))
            def _():
                push(block(z), block(z), at + z, b, 2 * to + c, at)

        stack(one)

    def line_relay(block, at):
        for middle, source, to in ((2, 1, 3), (1, 2, 0)):

            @pl.when(z == middle)
            def _():
                got(at + source, block(source))
                push(block(source), block(source), at + source, b, 2 * to + c, at)

    def line_got(block, at, k):
        here = (k == z) | ((z == 2) & (k == 1)) | ((z == 1) & (k == 2))

        @pl.when(jnp.logical_not(here))
        def _():
            got(at + k, block(0))

    lane = lax.broadcasted_iota(jnp.int32, (1, 128), 1)
    low = lane < 64
    own24 = pl.ds(pl.multiple_of(24 * c, 8), 24)
    mate24 = pl.ds(pl.multiple_of(24 * (1 - c), 8), 24)
    part = pl.ds(pl.multiple_of(HALF * c, 128), HALF)
    chip_rows = pl.ds(pl.multiple_of(48 * chip, 16), 48)
    group_rows = pl.ds(pl.multiple_of(192 * b, 16), 192)

    barrier = pltpu.get_barrier_semaphore()

    def greet(k):
        other = lax.rem(me + k, ALL)
        pl.semaphore_signal(
            barrier, inc=1, device_id=(lax.div(other, SEQ), lax.rem(other, SEQ)), device_id_type=MESH
        )

    loop(ALL, greet, 1)

    def natural(kind, p, head):
        return kind * WIDTH + 192 * p + 64 * head

    def half_at(ref, column, high):
        tile = ref[:, column // 128 * 128 : column // 128 * 128 + 128]
        return tile if (column % 128 == 64) == high else pltpu.roll(tile, 64, 1)

    for p in range(4):
        for tile in range(5):
            pair = []
            for high in (0, 1):
                which = HALVES[2 * tile + high]
                pair.append(
                    jnp.zeros((24, 128), F32)
                    if which is None
                    else half_at(i_wqkv, natural(which[0], p, which[1]), bool(high))
                )
            r.wide_qkv[own24, 768 * p + 128 * tile : 768 * p + 128 * tile + 128] = jnp.where(
                low, pair[0], pair[1]
            )
        r.wide_qkv[own24, 768 * p + 640 : 768 * p + 768] = jnp.zeros((24, 128), F32)
    r.wide_in[own24, :] = i_win[...]
    r.wide_attn[own24, :] = i_wattn[...]
    r.w_out[z, c] = i_wout[...].astype(BF)
    r.toks[z] = i_tok[0]
    lanes8 = lax.broadcasted_iota(jnp.int32, (8, 128), 1)
    half_cond = COND // 2
    speed = jnp.exp((lanes8 % half_cond).astype(F32) * (-math.log(10000.0) / half_cond))
    angle = i_when[0:1, :].astype(F32) * speed
    wave = jnp.where(lanes8 < half_cond, jnp.cos(angle), jnp.sin(angle))
    r.conds_all[b] = wave * (1.0 / (1.0 + jnp.exp(-wave)))
    pl.semaphore_wait(barrier, ALL - 1)

    def token_block(k):
        return r.toks.at[k]

    def in_block(k):
        return r.w_in.at[:, k, :, part]

    def out_block(k):
        return r.w_out.at[k, c]

    peers(lambda k, to: push(r.conds_all.at[b], r.conds_all.at[b], S.cond, to, s))
    sent(S.cond, r.conds_all.at[0:3])
    push(r.wide_qkv.at[own24], r.wide_qkv.at[own24], S.mix_qkv, b, mate)
    sent(S.mix_qkv, r.wide_qkv.at[0:24])
    push(r.wide_attn.at[own24], r.wide_attn.at[own24], S.mix_attn, b, mate)
    sent(S.mix_attn, r.wide_attn.at[0:24])
    push(r.wide_in.at[own24], r.wide_in.at[own24], S.mix_in, b, mate)
    sent(S.mix_in, r.wide_in.at[0:24])

    got(S.cond, r.conds_all.at[0:3])
    row8 = lax.broadcasted_iota(jnp.int32, (8, 128), 0)
    cond4 = jnp.zeros((8, 128), F32)
    for k in range(4):
        cond4 = jnp.where(row8 == k, r.conds_all[k], cond4)
    o_conds[...] = cond4
    wide = i_wada.shape[0]
    r.mod_pad[...] = jnp.zeros((8, 384), F32)
    r.mod_pad[:, 0:wide] = dot_nt(cond4.astype(BF), i_wada[...].astype(BF))
    columns = pltpu.roll(r.mod_pad[...], lax.rem(wide * me, 128), 1)
    for k in range(4):
        for t in range(3):
            r.mod_send[k, t : t + 1, :] = columns[k : k + 1, 128 * t : 128 * t + 128]
        r.mod_send[k, 3:4, :] = jnp.zeros((1, 128), F32)

    def send_mod(k):
        other = lax.rem(me + k, ALL)
        ob = lax.div(other, SEQ)
        push(r.mod_send.at[ob], r.mod_got.at[me], S.mod, ob, lax.rem(other, SEQ))

    loop(ALL, send_mod, 1)
    sent(S.mod, r.mod_got.at[0:31])
    keep(r.mod_send.at[b], r.mod_got.at[me], S.mod)

    def block(src, first):
        return src.at[:, pl.ds(pl.multiple_of(first, 128), HALF)]

    def along_line(src, dst, at, step):
        stack(
            lambda to: push(
                block(src, step * to + HALF * c), dst.at[chip_rows, part], at, b, 2 * to + c
            )
        )
        keep(block(src, step * z + HALF * c), dst.at[chip_rows, part], at)
        sent(at, dst.at[0:144, 0:HALF])

    def over_plane(dst, first, at):
        got(first, dst.at[0:192, 0:HALF])
        peers(
            lambda k, to: push(dst.at[group_rows, part], dst.at[group_rows, part], at, to, s)
        )
        sent(at, dst.at[0:576, 0:HALF])

    def share(dst, at, onward, rows):
        got(at, dst.at[0:rows, 0:HALF])
        push(dst.at[:, part], dst.at[:, part], onward, b, mate)
        sent(onward, dst.at[:, 0:HALF])

    got(S.mix_qkv, r.wide_qkv.at[0:24])
    r.s_qkv[...] = r.wide_qkv[...].astype(BF)
    along_line(r.s_qkv, r.w_qkv, S.w_qkv, WIDTH)
    line_gather(token_block, S.tok)
    sent(S.tok, r.toks.at[0:3])
    got(S.mix_attn, r.wide_attn.at[0:24])
    r.s_attn[...] = r.wide_attn[...].astype(BF)
    along_line(r.s_attn, r.w_attn, S.w_attn, 0)
    got(S.mix_in, r.wide_in.at[0:24])
    r.s_in[...] = r.wide_in[...].astype(BF)
    peers(
        lambda k, to: push(
            block(r.s_in, WIDTH * to + HALF * c), r.w_in.at[b, z, :, part], S.plane_in, to, s
        )
    )
    keep(block(r.s_in, WIDTH * b + HALF * c), r.w_in.at[b, z, :, part], S.plane_in)
    sent(S.plane_in, r.w_in.at[0:3, 0, :, 0:HALF])

    def start_tokens(tokens, k):
        place = (2 * k + c) * ROWS + lax.broadcasted_iota(jnp.int32, (ROWS, 1), 0)
        hidden = (place >= i_when[1:2, :]) & (place < i_when[1:2, :] + i_when[2:3, :])
        return jnp.where(hidden, i_vec[8:9, :], tokens.astype(F32)), hidden

    x0, _ = start_tokens(i_tok[0], z)
    r.x0[...] = x0
    n1, inv1 = normalize(x0)
    r.n1[...] = n1
    r.inv1[...] = jnp.broadcast_to(inv1, (ROWS, 128))

    got(S.mod, r.mod_got)
    r.mod_flat[...] = jnp.zeros((40, 128), F32)
    for k in range(ALL):
        first = 9 * k // 8
        r.mod_flat[first : first + 3, :] += r.mod_got[k, 0:3, :]
    for k in range(6):
        row = jnp.concatenate(
            [r.mod_flat[6 * k + t : 6 * k + t + 1, :] for t in range(6)], axis=1
        )
        r.mod[k : k + 1, :] = row + i_vec[2 + k : 3 + k, :]

    def mod(k):
        return r.mod[k : k + 1, :]

    def vec(k):
        return i_vec[k : k + 1, :]

    r.h1[z] = (r.n1[...] * vec(0) * (1.0 + mod(1)) + mod(0)).astype(BF)
    r.dm[0] = (i_cot[0].astype(F32) * mod(5)).astype(BF)
    over_plane(r.w_qkv, S.w_qkv, S.group_qkv)
    peers(lambda k, to: push(r.dm.at[0], r.dm.at[k], S.dm + k, to, s))
    for k in (1, 2, 3):
        sent(S.dm + k, r.dm.at[0])

    lanes = lax.broadcasted_iota(jnp.int32, (ROWS, 128), 1)
    first_half = lanes % HD < HD // 2
    speed = jnp.exp((lanes % (HD // 2)).astype(F32) * (-math.log(10000.0) / (HD // 2)))
    row = lax.broadcasted_iota(jnp.int32, (ROWS, 128), 0)

    def table(k):
        angle = ((2 * k + c) * ROWS + row).astype(F32) * speed
        r.turn[0, k] = jnp.cos(angle)
        sine = jnp.sin(angle)
        r.turn[1, k] = jnp.where(first_half, -sine, sine)

    loop(LINE, table)

    line_relay(token_block, S.tok)

    share(r.w_qkv, S.group_qkv, S.fw_qkv, 576)
    over_plane(r.w_attn, S.w_attn, S.group_attn)
    got(S.fw_qkv, r.w_qkv.at[:, 0:HALF])

    def turned(tile, sign, k):
        other = jnp.where(first_half, pltpu.roll(tile, 96, 1), pltpu.roll(tile, 32, 1))
        return tile * r.turn[0, k] + sign * (other * r.turn[1, k])

    def project(j):
        k = lax.rem(z + j, LINE)

        @pl.when(j > 0)
        def _():
            line_got(token_block, S.tok, k)
            other, _ = start_tokens(r.toks[k], k)
            other, _ = normalize(other)
            r.h1[k] = (other * vec(0) * (1.0 + mod(1)) + mod(0)).astype(BF)

        x = dot(r.h1[k], r.w_qkv[:, 0:PACK])
        tiles = [x[:, 128 * t : 128 * t + 128] for t in range(5)]
        tiles[0] = turned(tiles[0], 1.0, k) * 0.125
        tiles[1] = jnp.where(low, turned(tiles[1], 1.0, k) * 0.125, tiles[1])
        tiles[2] = turned(tiles[2], 1.0, k)
        tiles[3] = turned(tiles[3], 1.0, k)
        for t in range(5):
            r.xb[0, k, :, 128 * t : 128 * t + 128] = tiles[t].astype(BF)
        push(r.xb.at[0, k], r.xb.at[1, k], S.xf + k, b, mate)

    loop(4, project)
    for k in range(4):
        sent(S.xf + k, r.xb.at[0, 0])

    got(S.plane_in, r.w_in.at[:, 0, :, 0:HALF])
    line_gather(in_block, S.w_in)
    sent(S.w_in, r.w_in.at[0:3, :, :, 0:HALF])
    for k in range(4):
        got(S.xf + k, r.xb.at[0, 0])

    def tile_of(t):
        return r.xb[:, :, :, 128 * t : 128 * t + 128].reshape(1024, 128)

    heads = ((0, 2, 4, True, True), (0, 2, 4, False, False), (1, 3, 1, True, False))

    def queries(head, first, size):
        q_tile, _, _, q_low, _ = heads[head]
        q = r.xb[0, first : first + size, :, 128 * q_tile : 128 * q_tile + 128]
        return jnp.where(low if q_low else ~low, q.reshape(size * 128, 128), jnp.zeros((), BF))

    for half in range(2):
        at = slice(256 * half, 256 * half + 256)
        for head in range(3):
            scores = dot_nt(tile_of(heads[head][1]), queries(head, 2 * half, 2))
            weights = jnp.exp(scores - jnp.max(scores, axis=0, keepdims=True))
            weights = weights * (1.0 / jnp.sum(weights, axis=0, keepdims=True))
            weights = weights.astype(BF)
            r.pt[head, :, at] = weights
            out = dot_tn(tile_of(heads[head][2]), weights)
            if head == 0:
                r.ot[0, 0:64, at] = out[0:64]
            elif head == 1:
                r.ot[0, 64:128, at] = out[64:128]
            else:
                r.ot[1, 0:64, at] = out[64:128]
                r.ot[1, 64:128, at] = jnp.zeros((64, 256), F32)
        for t in range(2):
            r.os[2 * half : 2 * half + 2, :, 128 * t : 128 * t + 128] = (
                r.ot[t, :, at].T.astype(BF).reshape(2, 128, 128)
            )
        for to in (2 * half, 2 * half + 1):

            @pl.when(z == to)
            def _():
                keep(r.os.at[to], r.ob.at[z], S.o)

            @pl.when(z != to)
            def _():
                push(r.os.at[to], r.ob.at[z], S.o, b, 2 * to + c)

        if half == 0:
            line_relay(in_block, S.w_in)

    sent(S.o, r.os.at[0:3])
    line_gather(out_block, S.w_out)
    sent(S.w_out, r.w_out.at[0:3, 0])
    share(r.w_attn, S.group_attn, S.fw_attn, 576)
    got(S.fw_attn, r.w_attn.at[:, 0:HALF])
    got(S.o, r.ob)
    a = jnp.zeros((ROWS, WIDTH), F32)
    for p in range(4):
        a += dot(r.ob[p, :, 0:128], r.w_attn[192 * p : 192 * p + 128, :])
        a += dot(r.ob[p, :, 128:192], r.w_attn[192 * p + 128 : 192 * p + 192, :])
    r.a[...] = a
    x1 = r.x0[...] + mod(2) * a
    r.x1[...] = x1
    n2, inv2 = normalize(x1)
    r.n2[...] = n2
    r.inv2[...] = jnp.broadcast_to(inv2, (ROWS, 128))
    r.h2[0] = (n2 * vec(1) * (1.0 + mod(4)) + mod(3)).astype(BF)
    peers(lambda k, to: push(r.h2.at[0], r.h2.at[k], S.h2 + k, to, s))
    for k in (1, 2, 3):
        sent(S.h2 + k, r.h2.at[0])
    line_relay(out_block, S.w_out)
    for k in range(4):
        line_got(in_block, S.w_in, k)
    push(r.w_in.at[:, :, :, part], r.w_in.at[:, :, :, part], S.fw_in, b, mate)
    sent(S.fw_in, r.w_in.at[:, :, :, 0:HALF])
    for k in range(4):
        line_got(out_block, S.w_out, k)
    push(r.w_out.at[:, c], r.w_out.at[:, c], S.fw_out, b, mate)
    sent(S.fw_out, r.w_out.at[:, 0])
    got(S.fw_out, r.w_out.at[:, 0])
    got(S.fw_in, r.w_in.at[:, :, :, 0:HALF])

    def feed(first, count):
        at = slice(first, first + count)
        size = count * ROWS
        u = dot(r.h2[at].reshape(size, WIDTH), r.w_in[...].reshape(WIDTH, WIDTH))
        slope = 0.7978845608028654
        cube = 0.044715
        t = jnp.tanh(slope * (u + cube * u * u * u))
        r.gb[at] = (0.5 * u * (1.0 + t)).astype(BF).reshape(count, ROWS, WIDTH)
        bend = 0.5 * (1.0 + t) + 0.5 * u * (1.0 - t * t) * (slope * (1.0 + 3.0 * cube * u * u))
        back = dot_nt(r.dm[at].reshape(size, WIDTH), r.w_out[...].reshape(WIDTH, WIDTH))
        du = (back * bend).astype(BF)
        r.du[at] = du.reshape(count, ROWS, WIDTH)
        r.dhs[at] = dot_nt(du, r.w_in[...].reshape(WIDTH, WIDTH)).astype(BF).reshape(count, ROWS, WIDTH)

    feed(0, 1)
    for first, count in ((1, 2), (3, 1)):
        for k in range(first, first + count):
            got(S.h2 + k, r.h2.at[0])
            got(S.dm + k, r.dm.at[0])
        feed(first, count)
        for k in range(first, first + count):
            push(r.dhs.at[k], r.dhr.at[k], S.dh2, near[k], s)
    sent(S.dh2, r.dhs.at[0:3])
    for t in range(3):
        at = slice(256 * t, 256 * t + 256)
        mm = dot(r.gb[...].reshape(512, WIDTH), r.w_out[:, :, :, at].reshape(WIDTH, 256))
        r.mms[:, :, at] = mm.astype(BF).reshape(4, ROWS, 256)
    peers(lambda k, to: push(r.mms.at[k], r.mmr.at[k], S.mm, to, s))
    sent(S.mm, r.mms.at[0:3])

    def gather(own, others):
        total = own[0].astype(F32)
        for k in (1, 2, 3):
            total += others[k].astype(F32)
        return total

    for k in range(2):
        rows = slice(384 * k, 384 * k + 384)
        result = dot_tn(r.gb[:, :, rows].reshape(512, 384), r.dm[...].reshape(512, 768))
        r.g_out[2 * k : 2 * k + 2] = result.astype(BF).reshape(2, 2, 96, 768)
    push(r.g_out.at[:, 1 - c], r.p_out, S.pair_out, b, mate)
    sent(S.pair_out, r.p_out)

    def outer(left, right, dst):
        for k in range(2):
            rows = slice(384 * k, 384 * k + 384)
            result = dot_tn(
                left[:, :, rows].reshape(512, 384), right[...].reshape(512, 768)
            ).astype(BF)
            dst[0, rows, :] = result[:, 0:HALF]
            dst[1, rows, :] = result[:, HALF:WIDTH]

    def to_mate(grad, dst, at):
        push(grad.at[1 - c], dst, at, b, mate)
        sent(at, dst)

    def pair_sum(grad, pair, at):
        got(at, pair)
        grad[c] = (grad[c].astype(F32) + pair[...].astype(F32)).astype(BF)

    def plane_sum(grad, dst, at):
        def rows(to):
            return grad.at[c, pl.ds(pl.multiple_of(192 * to, 16), 192)]

        peers(lambda k, to: push(rows(to), dst.at[k], at, to, s))
        keep(rows(b), dst.at[0], at)
        sent(at, dst.at[0:3])

    def line_sum(src, total, dst, first, at):
        got(first, src)
        total[...] = (
            (src[0].astype(F32) + src[1].astype(F32)) + (src[2].astype(F32) + src[3].astype(F32))
        ).astype(BF)

        def rows(to):
            return total.at[pl.ds(pl.multiple_of(48 * to, 16), 48)]

        stack(lambda to: push(rows(to), dst.at[z], at, b, 2 * to + c))
        keep(rows(z), dst.at[z], at)
        sent(at, dst.at[0:3])

    def trade(total, final, at):
        push(total.at[:, mate24], final.at[:, c], at, b, mate)
        sent(at, final.at[:, 0])
        final[:, c] = total[:, own24, :]

    outer(r.h2, r.du, r.g_in)
    to_mate(r.g_in, r.p_in, S.pair_in)

    got(S.pair_out, r.p_out)
    for k in range(4):
        r.g_out[k, c] = (r.g_out[k, c].astype(F32) + r.p_out[k].astype(F32)).astype(BF)

    def send_gout(to):
        push(r.g_out.at[to, c], r.r_out.at[z], S.line_out, b, 2 * to + c)

    stack(send_gout)
    keep(r.g_out.at[z, c], r.r_out.at[z], S.line_out)
    sent(S.line_out, r.r_out.at[0:3])

    got(S.dh2, r.dhr.at[0:3])
    dh = gather(r.dhs, r.dhr)
    n2 = r.n2[...]
    inv2 = r.inv2[:, 0:1]
    r.early[...] = jnp.zeros((8, 768), F32)
    r.early[2:3, :] = jnp.sum(dh, axis=0, keepdims=True)
    both = jnp.sum(dh * n2, axis=0, keepdims=True)
    r.early[3:4, :] = both * vec(1)
    r.early[0:1, :] = both * (1.0 + mod(4))
    grad = dh * ((1.0 + mod(4)) * vec(1))
    dx1 = i_cot[0].astype(F32) + norm_back(n2, inv2, grad)
    r.dx1[...] = dx1
    r.early[1:2, :] = jnp.sum(dx1 * r.a[...], axis=0, keepdims=True)
    r.das[...] = (dx1 * mod(2)).astype(BF)
    for p in range(4):
        first = 192 * p
        r.dos[p, :, 0:128] = dot_nt(r.das[...], r.w_attn[first : first + 128, :]).astype(BF)
        tail = dot_nt(r.das[...], r.w_attn[first + 128 : first + 192, :])
        r.dos[p, :, 128:256] = jnp.concatenate(
            [tail, jnp.zeros((ROWS, 64), F32)], axis=1
        ).astype(BF)

    stack(lambda to: push(r.dos.at[to], r.dob.at[z], S.do, b, 2 * to + c))
    keep(r.dos.at[z], r.dob.at[z], S.do)
    sent(S.do, r.dos.at[0:3])

    for p in range(4):
        rows = slice(192 * p, 192 * p + 192)
        result = dot_tn(r.ob[p], r.das[...])[0:192].astype(BF)
        r.g_attn[0, rows, :] = result[:, 0:HALF]
        r.g_attn[1, rows, :] = result[:, HALF:WIDTH]
    to_mate(r.g_attn, r.p_attn, S.pair_attn)

    got(S.mm, r.mmr.at[0:3])
    mm = gather(r.mms, r.mmr)
    o_y[...] = (r.x1[...] + mod(5) * mm).astype(BF)
    r.early[4:5, :] = jnp.sum(i_cot[0].astype(F32) * mm, axis=0, keepdims=True)

    def over_line(src, dst, name):
        def one(k):
            push(src, dst.at[s], name, b, lax.rem(s + k, SEQ))

        loop(SEQ, one, 1)
        keep(src, dst.at[s], name)
        sent(name, dst.at[0:7])

    def over_group(got_ref, dst, name):
        total = got_ref[0]
        for k in range(1, SEQ):
            total += got_ref[k]
        dst[b] = total
        peers(lambda k, to: push(dst.at[b], dst.at[b], name, to, s))
        sent(name, dst.at[0:3])

    over_line(r.early, r.early_got, S.early)

    pair_sum(r.g_in, r.p_in, S.pair_in)

    def send_gin(k):
        to = lax.rem(chip + k, CHIPS)
        push(
            r.g_in.at[c, pl.ds(pl.multiple_of(48 * to, 16), 48)],
            r.r_in.at[chip],
            S.line_in,
            lax.div(to, LINE),
            2 * lax.rem(to, LINE) + c,
        )

    loop(CHIPS, send_gin, 1)
    keep(r.g_in.at[c, chip_rows], r.r_in.at[chip], S.line_in)
    sent(S.line_in, r.r_in.at[0:15])
    pair_sum(r.g_attn, r.p_attn, S.pair_attn)
    plane_sum(r.g_attn, r.q_attn, S.plane_attn)

    got(S.do, r.dob)
    dot0, dot1 = r.dob[:, :, 0:128].reshape(512, 128), r.dob[:, :, 128:256].reshape(512, 128)
    zero = jnp.zeros((), BF)
    moved = pltpu.roll(dot1.astype(F32), 64, 1).astype(BF)
    grads = (jnp.where(low, dot0, zero), jnp.where(low, zero, dot0), moved)
    product = dot0.astype(F32).T * r.ot[0]
    deltas = (
        jnp.sum(product[0:64], axis=0, keepdims=True),
        jnp.sum(product[64:128], axis=0, keepdims=True),
        jnp.sum(dot1.astype(F32).T * r.ot[1], axis=0, keepdims=True),
    )
    for head in range(3):
        values = tile_of(heads[head][2])
        for half in range(2):
            at = slice(256 * half, 256 * half + 256)
            dp = dot_nt(values, grads[head][at])
            r.dst[head, :, at] = (
                r.pt[head, :, at].astype(F32) * (dp - deltas[head][:, at])
            ).astype(BF)

    def key_grads(rows):
        dk = [dot(r.dst[head, rows, :], queries(head, 0, 4)) for head in range(3)]
        dv = [dot(r.pt[head, rows, :], grads[head]) for head in range(3)]
        return (dv[2], dk[0] + dk[1], dk[2], dv[0] + dv[1])

    for t, tile in enumerate(key_grads(slice(512, 1024))):
        r.gps[:, 128 * t : 128 * t + 128] = tile.astype(BF)
    push(r.gps, r.gpr, S.gp, b, mate)
    sent(S.gp, r.gps)
    for t, tile in enumerate(key_grads(slice(0, 512))):
        r.ga[:, 128 * t + 128 : 128 * t + 256] = tile
    for half in range(2):
        at = slice(256 * half, 256 * half + 256)
        turned_q = [dot_tn(tile_of(heads[head][1]), r.dst[head, :, at]) for head in range(3)]
        top = jnp.concatenate([turned_q[0][0:64], turned_q[1][64:128]], axis=0)
        r.ga[at, 0:128] = top.T * 0.125
        r.ga[at, 128:256] += turned_q[2].T * 0.125
    got(S.gp, r.gpr)

    def unproject(j):
        k = lax.rem(z + 1 + j, LINE)
        rows = pl.ds(pl.multiple_of(128 * k, 128), 128)
        tiles = [r.ga[rows, 0:128]] + [
            r.ga[rows, 128 * t : 128 * t + 128]
            + r.gpr[rows, 128 * t - 128 : 128 * t].astype(F32)
            for t in range(1, 5)
        ]
        tiles[0] = turned(tiles[0], -1.0, k)
        tiles[1] = jnp.where(low, turned(tiles[1], -1.0, k), tiles[1])
        tiles[2] = turned(tiles[2], -1.0, k)
        tiles[3] = turned(tiles[3], -1.0, k)
        for t in range(5):
            r.dqkv[k, :, 128 * t : 128 * t + 128] = tiles[t].astype(BF)
        r.dqkv[k, :, PACK:WIDTH] = jnp.zeros((128, 128), BF)
        r.d1s[k] = dot_nt(r.dqkv[k, :, 0:PACK], r.w_qkv[:, 0:PACK]).astype(BF)

        @pl.when(j < 3)
        def _():
            push(r.d1s.at[k], r.d1r.at[z], S.dh1, b, 2 * k + c)

    loop(4, unproject)
    sent(S.dh1, r.d1s.at[0:3])
    outer(r.h1, r.dqkv, r.g_qkv)
    to_mate(r.g_qkv, r.p_qkv, S.pair_qkv)
    line_sum(r.q_attn, r.m_attn, r.r_attn, S.plane_attn, S.line_attn)
    got(S.early, r.early_got)
    over_group(r.early_got, r.early_all, S.early2)
    pair_sum(r.g_qkv, r.p_qkv, S.pair_qkv)
    plane_sum(r.g_qkv, r.q_qkv, S.plane_qkv)

    got(S.line_in, r.r_in)
    for p in range(4):
        r.t_in[p] = (r.r_in[4 * p].astype(F32) + r.r_in[4 * p + 1].astype(F32)) + (
            r.r_in[4 * p + 2].astype(F32) + r.r_in[4 * p + 3].astype(F32)
        )
    trade(r.t_in, r.f_in, S.last_in)
    line_sum(r.q_qkv, r.m_qkv, r.r_qkv, S.plane_qkv, S.line_qkv)

    got(S.dh1, r.d1r.at[0:3])
    dh = r.d1s[z].astype(F32)
    for k in (1, 2, 3):
        dh += r.d1r[lax.rem(z + k, LINE)].astype(F32)
    n1 = r.n1[...]
    both = jnp.sum(dh * n1, axis=0, keepdims=True)
    r.late[0:1, :] = both * (1.0 + mod(1))
    r.late[1:2, :] = jnp.sum(dh, axis=0, keepdims=True)
    r.late[2:3, :] = both * vec(0)
    grad = dh * ((1.0 + mod(1)) * vec(0))
    dx0 = r.dx1[...] + norm_back(n1, r.inv1[:, 0:1], grad)
    _, hidden = start_tokens(i_tok[0], z)
    o_dx[...] = jnp.where(hidden, 0.0, dx0)
    r.late[3:4, :] = jnp.sum(jnp.where(hidden, dx0, 0.0), axis=0, keepdims=True)
    over_line(r.late, r.late_got, S.late)

    got(S.line_out, r.r_out)
    total = (r.r_out[0].astype(F32) + r.r_out[1].astype(F32)) + (
        r.r_out[2].astype(F32) + r.r_out[3].astype(F32)
    )
    o_gout[...] = total
    squares = total * total
    squares = jnp.sum(squares[:, 0:128] + squares[:, 128:256] + squares[:, 256:384]
                      + squares[:, 384:512] + squares[:, 512:640] + squares[:, 640:768],
                      axis=0, keepdims=True)

    def fold(value):
        total = value[:, 0:128] * value[:, 0:128]
        for t in range(1, value.shape[1] // 128):
            total += value[:, 128 * t : 128 * t + 128] * value[:, 128 * t : 128 * t + 128]
        return jnp.sum(total, axis=0, keepdims=True)

    got(S.line_attn, r.r_attn)
    r.t_attn[0] = (r.r_attn[0].astype(F32) + r.r_attn[1].astype(F32)) + (
        r.r_attn[2].astype(F32) + r.r_attn[3].astype(F32)
    )
    trade(r.t_attn, r.f_attn, S.last_attn)
    got(S.line_qkv, r.r_qkv)
    r.t_qkv[...] = r.r_qkv[...].astype(F32)
    trade(r.t_qkv, r.f_qkv, S.last_qkv)
    got(S.late, r.late_got)
    over_group(r.late_got, r.late_all, S.late2)
    got(S.last_in, r.f_in.at[:, 0])
    got(S.last_attn, r.f_attn.at[:, 0])
    for h in range(2):
        for p in range(4):
            value = r.f_in[p, h]
            o_gin[:, 768 * p + 384 * h : 768 * p + 384 * h + 384] = value
            squares += fold(value)
        value = r.f_attn[0, h]
        o_gattn[:, 384 * h : 384 * h + 384] = value
        squares += fold(value)
    got(S.last_qkv, r.f_qkv.at[:, 0])
    where = {which: index for index, which in enumerate(HALVES) if which is not None}

    def packed_half(chunk, high):
        kind, rest = chunk // 12, chunk % 12
        index = where[(kind, rest % 3)]
        t = index // 2
        tile = r.f_qkv[rest // 3, t // 3, :, t % 3 * 128 : t % 3 * 128 + 128]
        return tile if index % 2 == high else pltpu.roll(tile, 64, 1)

    for t in range(18):
        o_gqkv[:, 128 * t : 128 * t + 128] = jnp.where(
            low, packed_half(2 * t, 0), packed_half(2 * t + 1, 1)
        )
    for p in range(4):
        for h in range(2):
            squares += fold(r.f_qkv[p, h])

    r.sq[me] = squares

    def send_sq(k):
        other = lax.rem(me + k, ALL)
        push(r.sq.at[me], r.sq.at[me], S.sq, lax.div(other, SEQ), lax.rem(other, SEQ))

    loop(ALL, send_sq, 1)
    sent(S.sq, r.sq.at[0:31])
    got(S.early2, r.early_all.at[0:3])
    got(S.late2, r.late_all.at[0:3])
    mods = []
    for k in range(4):
        early, late = r.early_all[k], r.late_all[k]
        rows = jnp.concatenate([late[1:3], early[1:5], jnp.zeros((2, 768), F32)], axis=0)
        for n in range(6):
            for m in range(6):
                r.dmod_flat[k, 6 * n + m : 6 * n + m + 1, :] = rows[
                    n : n + 1, 128 * m : 128 * m + 128
                ]
        mods.append(rows)
    gain = jnp.concatenate(
        [
            sum(r.late_all[k][0:1] for k in range(4)),
            sum(r.early_all[k][0:1] for k in range(4)),
            (mods[0] + mods[1] + mods[2] + mods[3])[0:6],
        ],
        axis=0,
    )
    mask_row = sum(r.late_all[k][3:4] for k in range(4))
    gains = jnp.concatenate([gain, mask_row, jnp.zeros((7, 768), F32)], axis=0)
    masters = jnp.concatenate([i_vec[...], jnp.zeros((7, 768), F32)], axis=0)
    own = lax.rem(WIDTH - 24 * me, WIDTH)
    o_gvec[...] = pltpu.roll(gains, own, 1)[:, 0:128]
    o_vec[...] = pltpu.roll(masters, own, 1)[:, 0:128]
    r.mod_pad[...] = jnp.zeros((8, 384), F32)
    window = lax.div(wide * me, 128)
    for k in range(4):
        rows = r.dmod_flat[k, pl.ds(window, 3), :]
        for m in range(3):
            r.mod_pad[k : k + 1, 128 * m : 128 * m + 128] = rows[m : m + 1, :]
    o_dmod[...] = pltpu.roll(r.mod_pad[...], lax.rem(384 - lax.rem(wide * me, 128), 384), 1)[:, 0:256]
    small = jnp.sum(gain * gain) + jnp.sum(mask_row * mask_row)
    conds = [r.conds_all[k][0:1].astype(BF).astype(F32) for k in range(4)]
    for k in range(4):
        for m in range(k, 4):
            term = jnp.sum(mods[k] * mods[m]) * jnp.sum(conds[k] * conds[m])
            small += term if m == k else 2.0 * term
    got(S.sq, r.sq.at[0:31])
    total = r.sq[0]
    for k in range(1, ALL):
        total += r.sq[k]
    o_norm[...] = jnp.broadcast_to(jnp.sqrt(jnp.sum(total) + small), (8, 128))

    for at, like in drains:
        left(at, like)


def run_layer(*args):
    shapes = (
        ((ROWS, WIDTH), BF),
        ((ROWS, WIDTH), F32),
        ((8, 128), F32),
        ((24, 3 * WIDTH), F32),
        ((24, WIDTH), F32),
        ((24, 4 * WIDTH), F32),
        ((96, WIDTH), F32),
        ((8, 256), F32),
        ((16, 128), F32),
        ((16, 128), F32),
        ((8, 128), F32),
    )
    whole = pl.BlockSpec(memory_space=pltpu.VMEM)
    return pl.pallas_call(
        layer_kernel,
        out_shape=[jax.ShapeDtypeStruct(shape, kind) for shape, kind in shapes],
        in_specs=[whole] * len(args),
        out_specs=[whole] * len(shapes),
        scratch_shapes=[pltpu.VMEM(shape, kind) for shape, kind in SCRATCH.values()]
        + [pltpu.SemaphoreType.DMA((SEM_COUNT,)), pltpu.SemaphoreType.DMA((SEM_COUNT,))],
        compiler_params=pltpu.CompilerParams(
            collective_id=0, has_side_effects=True, vmem_limit_bytes=60 * 1024 * 1024
        ),
    )(*args)


def finish_kernel(
    y, dx, norm, g_qkv, g_attn, g_in, g_out, dmod, g_vec, own_vec, conds, *rest
):
    (w_ada, w_qkv, w_attn, w_in, w_out), moments, outs = rest[:5], rest[5:17], rest[17:]
    outs[0][0] = y[...]
    outs[1][0] = dx[...]
    outs[2][0, 0] = norm[0, 0]
    clip = jnp.minimum(1.0, CLIP / (norm[0:1, 0:1] + 1e-06))
    columns = w_ada.shape[0]
    rounded = conds[...].astype(BF).astype(F32)
    turned_mod = dmod[...].T
    g_ada = turned_mod[0:columns, 0:1] * rounded[0:1, :]
    for k in range(1, 4):
        g_ada += turned_mod[0:columns, k : k + 1] * rounded[k : k + 1, :]
    narrow = moments[0].shape[1]
    grads = (
        g_vec[0:9, 0:narrow],
        g_ada,
        g_qkv[...],
        g_attn[...],
        g_in[...],
        g_out[...],
    )
    weights = (
        own_vec[0:9, 0:narrow],
        w_ada[...],
        w_qkv[...],
        w_attn[...],
        w_in[...],
        w_out[...],
    )
    for k in range(6):
        results = adam_step(
            weights[k],
            grads[k] * clip,
            moments[2 * k][...],
            moments[2 * k + 1][...],
            RATE if k else RATE_VECTORS,
            DECAY if k else 0.0,
        )
        for n in range(3):
            outs[3 + 3 * k + n][...] = results[n]


def run_finish(partial_results, weights, moments):
    shapes = [((1, ROWS, WIDTH), BF), ((1, ROWS, WIDTH), F32), ((1, 1), F32)]
    for moment in moments[::2]:
        shapes += [(moment.shape, F32)] * 3
    whole = pl.BlockSpec(memory_space=pltpu.VMEM)
    specs = [whole] * len(shapes)
    specs[2] = pl.BlockSpec(memory_space=pltpu.SMEM)
    args = (*partial_results, *weights, *moments)
    return pl.pallas_call(
        finish_kernel,
        out_shape=[jax.ShapeDtypeStruct(shape, kind) for shape, kind in shapes],
        in_specs=[whole] * len(args),
        out_specs=specs,
        compiler_params=pltpu.CompilerParams(vmem_limit_bytes=60 * 1024 * 1024),
    )(*args)


def slices(
    tokens_in,
    cotangent,
    timesteps,
    span_start,
    span_len,
    vectors,
    w_ada,
    w_qkv,
    w_attn,
    w_in,
    w_out,
    m_vec,
    v_vec,
    m_ada,
    v_ada,
    m_qkv,
    v_qkv,
    m_attn,
    v_attn,
    m_in,
    v_in,
    m_out,
    v_out,
):
    partial_results = run_layer(
        jnp.stack([timesteps, span_start, span_len]),
        tokens_in,
        cotangent,
        vectors,
        w_ada.T,
        w_qkv,
        w_attn,
        w_in,
        w_out,
    )
    moments = (
        m_vec,
        v_vec,
        m_ada.T,
        v_ada.T,
        m_qkv,
        v_qkv,
        m_attn,
        v_attn,
        m_in,
        v_in,
        m_out,
        v_out,
    )
    results = run_finish(partial_results, (w_ada.T, w_qkv, w_attn, w_in, w_out), moments)
    ada_results = [result.T for result in results[6:9]]
    return (*results[:2], results[2].reshape(()), *results[3:6], *ada_results, *results[9:])


def solution(mesh):
    in_specs = (
        P("dp", "seq", None),
        P("dp", "seq", None),
        P("dp"),
        P("dp"),
        P("dp"),
        P(),
        P(None, ("dp", "seq")),
        P(("dp", "seq"), None),
        P(("dp", "seq"), None),
        P(("dp", "seq"), None),
        P(("dp", "seq"), None),
        P(None, ("dp", "seq")),
        P(None, ("dp", "seq")),
        P(None, ("dp", "seq")),
        P(None, ("dp", "seq")),
        P(("dp", "seq"), None),
        P(("dp", "seq"), None),
        P(("dp", "seq"), None),
        P(("dp", "seq"), None),
        P(("dp", "seq"), None),
        P(("dp", "seq"), None),
        P(("dp", "seq"), None),
        P(("dp", "seq"), None),
    )
    out_specs = (
        P("dp", "seq", None),
        P("dp", "seq", None),
        P(),
        P(None, ("dp", "seq")),
        P(None, ("dp", "seq")),
        P(None, ("dp", "seq")),
        P(None, ("dp", "seq")),
        P(None, ("dp", "seq")),
        P(None, ("dp", "seq")),
        P(("dp", "seq"), None),
        P(("dp", "seq"), None),
        P(("dp", "seq"), None),
        P(("dp", "seq"), None),
        P(("dp", "seq"), None),
        P(("dp", "seq"), None),
        P(("dp", "seq"), None),
        P(("dp", "seq"), None),
        P(("dp", "seq"), None),
        P(("dp", "seq"), None),
        P(("dp", "seq"), None),
        P(("dp", "seq"), None),
    )
    sizes = dict(mesh.shape)
    local = slices if (sizes["dp"], sizes["seq"]) == (4, 8) else plain
    return jax.shard_map(local, mesh=mesh, in_specs=in_specs, out_specs=out_specs, check_vma=False)
```

```python
from functools import partial
import math
from types import SimpleNamespace

import jax
import jax.numpy as jnp
from jax import lax
from jax.experimental import pallas as pl
from jax.experimental.pallas import tpu as pltpu
from jax.sharding import PartitionSpec as P

HD = 64
COND = 128
STEP = 10


BETA_ONE = 0.9
BETA_TWO = 0.999
ADAM_EPS = 1e-08
RATE = 0.1
RATE_VECTORS = 0.3
DECAY = 0.01
CLIP = 1.0
NORM_EPS = 1e-05


def cond_input(timesteps):
    half_cond = COND // 2
    freqs = jnp.exp(jnp.arange(half_cond, dtype=jnp.float32) * (-math.log(10000.0) / half_cond))
    angles = timesteps.astype(jnp.float32)[:, None] * freqs[None, :]
    return jax.nn.silu(jnp.concatenate([jnp.cos(angles), jnp.sin(angles)], axis=1))


def rotary_tables(positions):
    half_head = HD // 2
    inverse = jnp.exp(jnp.arange(half_head, dtype=jnp.float32) * (-math.log(10000.0) / half_head))
    angles = positions.astype(jnp.float32)[:, None] * inverse[None, :]
    return (jnp.cos(angles), jnp.sin(angles))


def rotate(values, cosines, sines):
    half_head = values.shape[-1] // 2
    first = values[..., :half_head]
    second = values[..., half_head:]
    cos_b = cosines[:, None, :]
    sin_b = sines[:, None, :]
    return jnp.concatenate(
        [first * cos_b - second * sin_b, second * cos_b + first * sin_b], axis=-1
    )


def rotate_back(grads, cosines, sines):
    half_head = grads.shape[-1] // 2
    first = grads[..., :half_head]
    second = grads[..., half_head:]
    cos_b = cosines[:, None, :]
    sin_b = sines[:, None, :]
    return jnp.concatenate(
        [first * cos_b + second * sin_b, second * cos_b - first * sin_b], axis=-1
    )


def normalize(values):
    centre = jnp.mean(values, axis=-1, keepdims=True)
    centred = values - centre
    inverse = lax.rsqrt(jnp.mean(centred * centred, axis=-1, keepdims=True) + NORM_EPS)
    return (centred * inverse, inverse)


def norm_back(normed, inverse, grad):
    return inverse * (
        grad
        - jnp.mean(grad, axis=-1, keepdims=True)
        - normed * jnp.mean(grad * normed, axis=-1, keepdims=True)
    )


def split_kv(block, width):
    seqs, block_rows = (block.shape[0], block.shape[1])
    keys = block[..., :width].reshape(seqs, block_rows, width // HD, HD)
    values = block[..., width:].reshape(seqs, block_rows, width // HD, HD)
    return (keys, values)


def attend_piece(carry, piece, queries, width, factor):
    piece_rows = piece.shape[1]
    size = math.gcd(piece_rows, 512)

    def attend_one_block(index, state):
        running, denom, accum = state
        block = lax.dynamic_slice_in_dim(piece, index * size, size, 1)
        keys, values = split_kv(block, width)
        scores = (
            jnp.einsum("sqhd,skhd->shqk", queries, keys, preferred_element_type=jnp.float32)
            * factor
        )
        highest = jnp.maximum(running, jnp.max(scores, axis=-1))
        shrink = jnp.exp(running - highest)
        weights = jnp.exp(scores - highest[..., None])
        denom = denom * shrink + jnp.sum(weights, axis=-1)
        accum = accum * shrink[..., None] + jnp.einsum(
            "shqk,skhd->shqd",
            weights.astype(jnp.bfloat16),
            values,
            preferred_element_type=jnp.float32,
        )
        return (highest, denom, accum)

    return lax.fori_loop(0, piece_rows // size, attend_one_block, carry)


def block_grads(block, queries, grad_out, logsum, delta, width, factor):
    keys, values = split_kv(block, width)
    scores = (
        jnp.einsum("sqhd,skhd->shqk", queries, keys, preferred_element_type=jnp.float32) * factor
    )
    probs = jnp.exp(scores - logsum[..., None])
    dprobs = jnp.einsum("sqhd,skhd->shqk", grad_out, values, preferred_element_type=jnp.float32)
    dscores = (probs * (dprobs - delta[..., None])).astype(jnp.bfloat16)
    return (keys, probs, dscores)


def query_grads(kv_all, queries, grad_out, logsum, delta, width, factor):
    total_rows = kv_all.shape[1]
    size = math.gcd(total_rows, 512)

    def query_one_block(index, accum):
        block = lax.dynamic_slice_in_dim(kv_all, index * size, size, 1)
        keys, probs, dscores = block_grads(block, queries, grad_out, logsum, delta, width, factor)
        return accum + factor * jnp.einsum(
            "shqk,skhd->sqhd", dscores, keys, preferred_element_type=jnp.float32
        )

    return lax.fori_loop(
        0, total_rows // size, query_one_block, jnp.zeros(queries.shape, jnp.float32)
    )


def key_grads(kv_all, queries, grad_out, logsum, delta, width, factor, count):
    size = math.gcd(count, 512)
    seqs = queries.shape[0]

    def key_one_block(index, accum):
        block = lax.dynamic_slice_in_dim(kv_all, index * size, size, 1)
        keys, probs, dscores = block_grads(block, queries, grad_out, logsum, delta, width, factor)
        grad_vals = jnp.einsum(
            "shqk,sqhd->skhd",
            probs.astype(jnp.bfloat16),
            grad_out,
            preferred_element_type=jnp.float32,
        )
        grad_keys = factor * jnp.einsum(
            "shqk,sqhd->skhd", dscores, queries, preferred_element_type=jnp.float32
        )
        joined = jnp.concatenate(
            [grad_keys.reshape(seqs, size, width), grad_vals.reshape(seqs, size, width)], axis=-1
        )
        return lax.dynamic_update_slice_in_dim(
            accum, jnp.transpose(joined, (1, 0, 2)), index * size, 0
        )

    initial = jnp.zeros((count, seqs, 2 * width), jnp.float32)
    return lax.fori_loop(0, count // size, key_one_block, initial)


def adam_step(weight, grad, first, second, rate, decay_rate):
    new_first = BETA_ONE * first + (1.0 - BETA_ONE) * grad
    new_second = BETA_TWO * second + (1.0 - BETA_TWO) * grad * grad
    fixed_first = new_first / (1.0 - BETA_ONE**STEP)
    fixed_second = new_second / (1.0 - BETA_TWO**STEP)
    new_weight = weight - rate * (
        fixed_first / (jnp.sqrt(fixed_second) + ADAM_EPS) + decay_rate * weight
    )
    return (new_first, new_second, new_weight)


def mod_back(grad_hidden, ln_values, normed, scale_part, gain):
    grad_shift = jnp.sum(grad_hidden, axis=1)
    grad_scale = jnp.sum(grad_hidden * ln_values, axis=1)
    grad_ln = grad_hidden * (1.0 + scale_part)
    grad_gain = jnp.sum(grad_ln * normed, axis=(0, 1))
    return (grad_shift, grad_scale, grad_gain, grad_ln * gain)


def plain(
    tokens_in,
    cotangent,
    timesteps,
    span_start,
    span_len,
    vectors,
    w_ada,
    w_qkv,
    w_attn,
    w_in,
    w_out,
    m_vec,
    v_vec,
    m_ada,
    v_ada,
    m_qkv,
    v_qkv,
    m_attn,
    v_attn,
    m_in,
    v_in,
    m_out,
    v_out,
):
    seqs, group, width = tokens_in.shape
    heads = width // HD
    factor = HD ** (-0.5)
    flat_rows = seqs * group
    full_ada, full_qkv, full_attn, full_in, full_out = (
        lax.all_gather(w_ada.astype(jnp.bfloat16), ("dp", "seq"), axis=1, tiled=True),
        lax.all_gather(w_qkv.astype(jnp.bfloat16), ("dp", "seq"), axis=0, tiled=True),
        lax.all_gather(w_attn.astype(jnp.bfloat16), ("dp", "seq"), axis=0, tiled=True),
        lax.all_gather(w_in.astype(jnp.bfloat16), ("dp", "seq"), axis=0, tiled=True),
        lax.all_gather(w_out.astype(jnp.bfloat16), ("dp", "seq"), axis=0, tiled=True),
    )
    positions = lax.axis_index("seq") * group + jnp.arange(group, dtype=jnp.int32)
    masked = (positions[None, :] >= span_start[:, None]) & (
        positions[None, :] < (span_start + span_len)[:, None]
    )
    cond_bf = cond_input(timesteps).astype(jnp.bfloat16)
    modulation = jnp.dot(cond_bf, full_ada, preferred_element_type=jnp.float32) + vectors[
        2:8
    ].reshape(1, 6 * width)
    pieces = [modulation[:, which * width : (which + 1) * width][:, None, :] for which in range(6)]
    shift_one, scale_one, gate_one, shift_two, scale_two, gate_two = pieces
    start_tokens = jnp.where(
        masked[..., None], vectors[8][None, None, :], tokens_in.astype(jnp.float32)
    )
    normed_one, inv_one = normalize(start_tokens)
    ln_one = normed_one * vectors[0]
    hidden_one = (
        (ln_one * (1.0 + scale_one) + shift_one).astype(jnp.bfloat16).reshape(flat_rows, width)
    )
    projected = jnp.dot(hidden_one, full_qkv, preferred_element_type=jnp.float32).reshape(
        seqs, group, 3 * width
    )
    cosines, sines = rotary_tables(positions)
    queries = rotate(projected[..., :width].reshape(seqs, group, heads, HD), cosines, sines).astype(
        jnp.bfloat16
    )
    keys_here = rotate(
        projected[..., width : 2 * width].reshape(seqs, group, heads, HD), cosines, sines
    ).astype(jnp.bfloat16)
    values_here = projected[..., 2 * width :].astype(jnp.bfloat16)
    kv_local = jnp.concatenate([keys_here.reshape(seqs, group, width), values_here], axis=-1)
    initial = (
        jnp.full((seqs, heads, group), -1e30, jnp.float32),
        jnp.zeros((seqs, heads, group), jnp.float32),
        jnp.zeros((seqs, heads, group, HD), jnp.float32),
    )
    running, denom, accum = attend_piece(
        initial, lax.all_gather(kv_local, "seq", axis=1, tiled=True), queries, width, factor
    )
    attn_heads = accum / denom[..., None]
    logsum = running + jnp.log(denom)
    attn_rows = jnp.transpose(attn_heads, (0, 2, 1, 3)).reshape(flat_rows, width)
    attn_bf = attn_rows.astype(jnp.bfloat16)
    branch_one = jnp.dot(attn_bf, full_attn, preferred_element_type=jnp.float32).reshape(
        seqs, group, width
    )
    mid_tokens = start_tokens + gate_one * branch_one
    normed_two, inv_two = normalize(mid_tokens)
    ln_two = normed_two * vectors[1]
    hidden_two = (
        (ln_two * (1.0 + scale_two) + shift_two).astype(jnp.bfloat16).reshape(flat_rows, width)
    )
    pre_act = jnp.dot(hidden_two, full_in, preferred_element_type=jnp.float32)
    activ, gelu_back = jax.vjp(partial(jax.nn.gelu, approximate=True), pre_act)
    activ_bf = activ.astype(jnp.bfloat16)
    branch_two = jnp.dot(activ_bf, full_out, preferred_element_type=jnp.float32).reshape(
        seqs, group, width
    )
    block_out = (mid_tokens + gate_two * branch_two).astype(jnp.bfloat16)
    grad_y = cotangent.astype(jnp.float32)
    grad_gate_two = jnp.sum(grad_y * branch_two, axis=1)
    grad_branch_two = (grad_y * gate_two).astype(jnp.bfloat16).reshape(flat_rows, width)
    grad_w_out = jnp.dot(activ_bf.T, grad_branch_two, preferred_element_type=jnp.float32)
    grad_activ = jnp.dot(grad_branch_two, full_out.T, preferred_element_type=jnp.float32)
    grad_pre = gelu_back(grad_activ)[0].astype(jnp.bfloat16)
    grad_w_in = jnp.dot(hidden_two.T, grad_pre, preferred_element_type=jnp.float32)
    grad_hidden_two = jnp.dot(grad_pre, full_in.T, preferred_element_type=jnp.float32).reshape(
        seqs, group, width
    )
    grad_shift_two, grad_scale_two, grad_gain_two, grad_normed_two = mod_back(
        grad_hidden_two, ln_two, normed_two, scale_two, vectors[1]
    )
    grad_mid = grad_y + norm_back(normed_two, inv_two, grad_normed_two)
    grad_gate_one = jnp.sum(grad_mid * branch_one, axis=1)
    grad_branch_one = (grad_mid * gate_one).astype(jnp.bfloat16).reshape(flat_rows, width)
    grad_w_attn = jnp.dot(attn_bf.T, grad_branch_one, preferred_element_type=jnp.float32)
    grad_attn_bf = (
        jnp.dot(grad_branch_one, full_attn.T, preferred_element_type=jnp.float32)
        .astype(jnp.bfloat16)
        .reshape(seqs, group, heads, HD)
    )
    delta = jnp.einsum("sqhd,shqd->shq", grad_attn_bf.astype(jnp.float32), attn_heads)
    kv_all = lax.all_gather(kv_local, "seq", axis=1, tiled=True)
    grad_queries = query_grads(kv_all, queries, grad_attn_bf, logsum, delta, width, factor)
    grad_kv = jnp.transpose(
        lax.psum_scatter(
            key_grads(
                kv_all,
                queries,
                grad_attn_bf,
                logsum,
                delta,
                width,
                factor,
                group * lax.axis_size("seq"),
            ).astype(jnp.bfloat16),
            "seq",
            scatter_dimension=0,
            tiled=True,
        ).astype(jnp.float32),
        (1, 0, 2),
    )
    grad_keys = grad_kv[..., :width].reshape(seqs, group, heads, HD)
    grad_qkv = jnp.concatenate(
        [
            rotate_back(grad_queries, cosines, sines).reshape(seqs, group, width),
            rotate_back(grad_keys, cosines, sines).reshape(seqs, group, width),
            grad_kv[..., width:],
        ],
        axis=-1,
    )
    grad_qkv = grad_qkv.astype(jnp.bfloat16).reshape(flat_rows, 3 * width)
    grad_w_qkv = jnp.dot(hidden_one.T, grad_qkv, preferred_element_type=jnp.float32)
    grad_hidden_one = jnp.dot(grad_qkv, full_qkv.T, preferred_element_type=jnp.float32).reshape(
        seqs, group, width
    )
    grad_shift_one, grad_scale_one, grad_gain_one, grad_normed_one = mod_back(
        grad_hidden_one, ln_one, normed_one, scale_one, vectors[0]
    )
    grad_start = grad_mid + norm_back(normed_one, inv_one, grad_normed_one)
    grad_mask_row = jnp.sum(jnp.where(masked[..., None], grad_start, 0.0), axis=(0, 1))
    grad_input = jnp.where(masked[..., None], 0.0, grad_start)
    grad_mod = jnp.concatenate(
        [
            grad_shift_one,
            grad_scale_one,
            grad_gate_one,
            grad_shift_two,
            grad_scale_two,
            grad_gate_two,
        ],
        axis=1,
    )
    grad_w_ada = jnp.dot(cond_bf.astype(jnp.float32).T, grad_mod, precision=lax.Precision.HIGHEST)
    grad_vectors = jnp.concatenate(
        [
            grad_gain_one[None, :],
            grad_gain_two[None, :],
            jnp.sum(grad_mod, axis=0).reshape(6, width),
            grad_mask_row[None, :],
        ],
        axis=0,
    )
    red_ada, red_qkv, red_attn, red_in, red_out, red_vec = (
        lax.psum_scatter(grad_w_ada, ("dp", "seq"), scatter_dimension=1, tiled=True),
        lax.psum_scatter(grad_w_qkv, ("dp", "seq"), scatter_dimension=0, tiled=True),
        lax.psum_scatter(grad_w_attn, ("dp", "seq"), scatter_dimension=0, tiled=True),
        lax.psum_scatter(grad_w_in, ("dp", "seq"), scatter_dimension=0, tiled=True),
        lax.psum_scatter(grad_w_out, ("dp", "seq"), scatter_dimension=0, tiled=True),
        lax.psum_scatter(grad_vectors, ("dp", "seq"), scatter_dimension=1, tiled=True),
    )
    local_squares = jnp.float32(0.0)
    for reduced in (red_vec, red_ada, red_qkv, red_attn, red_in, red_out):
        local_squares = local_squares + jnp.sum(reduced * reduced)
    grad_norm = jnp.sqrt(lax.psum(local_squares, ("dp", "seq")))
    clip_factor = jnp.minimum(1.0, CLIP / (grad_norm + 1e-06))
    columns = red_vec.shape[1]
    own_vectors = lax.dynamic_slice_in_dim(
        vectors, lax.axis_index(("dp", "seq")) * columns, columns, 1
    )
    vec_out = adam_step(own_vectors, red_vec * clip_factor, m_vec, v_vec, RATE_VECTORS, 0.0)
    ada_out = adam_step(w_ada, red_ada * clip_factor, m_ada, v_ada, RATE, DECAY)
    qkv_out = adam_step(w_qkv, red_qkv * clip_factor, m_qkv, v_qkv, RATE, DECAY)
    attn_out = adam_step(w_attn, red_attn * clip_factor, m_attn, v_attn, RATE, DECAY)
    in_out = adam_step(w_in, red_in * clip_factor, m_in, v_in, RATE, DECAY)
    out_out = adam_step(w_out, red_out * clip_factor, m_out, v_out, RATE, DECAY)
    return (
        block_out,
        grad_input,
        grad_norm,
        vec_out[0],
        vec_out[1],
        vec_out[2],
        ada_out[0],
        ada_out[1],
        ada_out[2],
        qkv_out[0],
        qkv_out[1],
        qkv_out[2],
        attn_out[0],
        attn_out[1],
        attn_out[2],
        in_out[0],
        in_out[1],
        in_out[2],
        out_out[0],
        out_out[1],
        out_out[2],
    )


F32, BF = jnp.float32, jnp.bfloat16
MESH = pl.DeviceIdType.MESH
DP, LINE, SEQ, CHIPS, ALL = 4, 4, 8, 16, 32
ROWS, WIDTH, PACK = 128, 768, 640
HALF = WIDTH // 2
HALVES = ((0, 0), (0, 1), (0, 2), (2, 2), (1, 0), (1, 1), (1, 2), None, (2, 0), (2, 1))

def numbered(**counts):
    at = {}
    for name, count in counts.items():
        at[name] = sum(counts[other] for other in at)
    return SimpleNamespace(**at), sum(counts.values())


S, SEM_COUNT = numbered(
    when=3,
    cond=1,
    mix_qkv=1,
    mix_in=1,
    mix_attn=1,
    mod=1,
    w_qkv=1,
    w_attn=1,
    plane_in=1,
    w_in=4,
    w_out=4,
    group_qkv=1,
    group_attn=1,
    fw_qkv=1,
    fw_attn=1,
    fw_in=1,
    fw_out=1,
    tok=4,
    h2=4,
    dm=4,
    xf=4,
    o=1,
    mm=1,
    dh2=1,
    do=1,
    gp=1,
    dh1=5,
    pair_out=1,
    pair_in=1,
    pair_attn=1,
    pair_qkv=1,
    plane_attn=1,
    plane_qkv=1,
    line_out=5,
    line_in=5,
    slice_in=1,
    line_attn=1,
    line_qkv=1,
    last_in=1,
    last_attn=1,
    last_qkv=1,
    early=1,
    early2=1,
    late=1,
    late2=1,
    sq=1,
)

SCRATCH = dict(
    wide_qkv=((48, 3072), F32),
    wide_in=((48, 3072), F32),
    wide_attn=((48, 768), F32),
    s_qkv=((48, 3072), BF),
    s_in=((48, 3072), BF),
    s_attn=((48, 768), BF),
    w_qkv=((768, 768), BF),
    w_in=((4, 4, 48, 768), BF),
    w_attn=((768, 768), BF),
    w_out=((4, 2, 96, 768), BF),
    conds_all=((4, 8, 128), F32),
    mod_send=((4, 4, 128), F32),
    mod_got=((32, 4, 128), F32),
    mod_flat=((40, 128), F32),
    mod_pad=((8, 384), F32),
    turn=((2, 4, 128, 128), F32),
    dmod_flat=((4, 40, 128), F32),
    mod=((8, 768), F32),
    x0=((128, 768), F32),
    n1=((128, 768), F32),
    inv1=((128, 128), F32),
    x1=((128, 768), F32),
    n2=((128, 768), F32),
    inv2=((128, 128), F32),
    a=((128, 768), F32),
    dx1=((128, 768), F32),
    toks=((4, 128, 768), BF),
    h1=((4, 128, 768), BF),
    h2=((4, 128, 768), BF),
    dm=((4, 128, 768), BF),
    gb=((4, 128, 768), BF),
    du=((4, 128, 768), BF),
    xb=((2, 4, 128, 640), BF),
    pt=((3, 1024, 512), BF),
    ot=((2, 128, 512), F32),
    os=((4, 128, 256), BF),
    ob=((4, 128, 256), BF),
    mms=((4, 128, 768), BF),
    mmr=((4, 128, 768), BF),
    dhs=((4, 128, 768), BF),
    dhr=((4, 128, 768), BF),
    das=((128, 768), BF),
    dos=((4, 128, 256), BF),
    dob=((4, 128, 256), BF),
    dst=((3, 1024, 512), BF),
    ga=((512, 640), F32),
    gps=((512, 512), BF),
    gpr=((512, 512), BF),
    dqkv=((4, 128, 768), BF),
    d1s=((4, 128, 768), BF),
    d1r=((4, 128, 768), BF),
    g_out=((4, 2, 96, 768), BF),
    g_in=((2, 4, 4, 48, 384), BF),
    g_attn=((2, 768, 384), BF),
    g_qkv=((2, 768, 384), BF),
    p_out=((4, 96, 768), BF),
    p_in=((4, 4, 48, 384), BF),
    p_attn=((768, 384), BF),
    p_qkv=((768, 384), BF),
    q_attn=((4, 192, 384), BF),
    q_qkv=((4, 192, 384), BF),
    m_attn=((192, 384), BF),
    m_qkv=((192, 384), BF),
    r_out=((4, 96, 768), BF),
    r_in=((4, 4, 48, 384), BF),
    via_in=((4, 48, 384), BF),
    via_out=((96, 768), BF),
    via_dh1=((128, 768), BF),
    m_in=((4, 48, 384), BF),
    u_in=((4, 48, 384), BF),
    r_attn=((4, 48, 384), BF),
    r_qkv=((4, 48, 384), BF),
    t_in=((4, 48, 384), F32),
    t_attn=((1, 48, 384), F32),
    t_qkv=((4, 48, 384), F32),
    f_in=((4, 2, 24, 384), F32),
    f_attn=((1, 2, 24, 384), F32),
    f_qkv=((4, 2, 24, 384), F32),
    early=((8, 768), F32),
    early_got=((8, 8, 768), F32),
    early_all=((4, 8, 768), F32),
    late=((4, 768), F32),
    late_got=((8, 4, 768), F32),
    late_all=((4, 4, 768), F32),
    sq=((32, 1, 128), F32),
)


def dot(left, right):
    return jnp.dot(left, right, preferred_element_type=F32)


def dot_nt(left, right):
    return lax.dot_general(left, right, (((1,), (1,)), ((), ())), preferred_element_type=F32)


def dot_tn(left, right):
    return lax.dot_general(left, right, (((0,), (0,)), ((), ())), preferred_element_type=F32)


def loop(count, body, start=0):
    def step(index, carry):
        body(index)
        return carry

    lax.fori_loop(start, count, step, 0)


def layer_kernel(
    i_time,
    i_start,
    i_len,
    i_tok,
    i_cot,
    i_vec,
    i_wada,
    i_wqkv,
    i_wattn,
    i_win,
    i_wout,
    o_y,
    o_dx,
    o_norm,
    o_gqkv,
    o_gattn,
    o_gin,
    o_gout,
    o_dmod,
    o_gvec,
    o_vec,
    o_conds,
    *scratch,
):
    r = SimpleNamespace(**dict(zip(SCRATCH, scratch)), when=scratch[-3])
    send_sems, recv_sems = scratch[-2:]
    b, s = lax.axis_index("dp"), lax.axis_index("seq")
    z, c = lax.div(s, 2), lax.rem(s, 2)
    mate = s + 1 - 2 * c
    chip = b * LINE + z
    me = b * SEQ + s
    drains = []

    def push(src, dst, at, to_b, to_s, out=None):
        pltpu.make_async_remote_copy(
            src_ref=src,
            dst_ref=dst,
            send_sem=send_sems.at[at if out is None else out],
            recv_sem=recv_sems.at[at],
            device_id=(to_b, to_s),
            device_id_type=MESH,
        ).start()

    def keep(src, dst, at):
        pltpu.make_async_copy(src, dst, recv_sems.at[at]).start()

    def got(at, like):
        pltpu.make_async_copy(like, like, recv_sems.at[at]).wait()

    def left(at, like):
        pltpu.make_async_copy(like, like, send_sems.at[at]).wait()

    def sent(at, like):
        drains.append((at, like))

    near = (b, b + 1 - 2 * lax.rem(b, 2), b + 2 - 4 * lax.div(b, 2), 3 - b)

    def peers(body):
        for k in (1, 2, 3):
            body(k, near[k])

    def stack(body):
        for k in (1, 2, 3):
            body(lax.rem(z + k, LINE))

    def line_gather(block, at):
        def one(to):
            @pl.when(jnp.logical_not(((z == 1) & (to == 3)) | ((z == 2) & (to == 0))))
            def _():
                push(block(z), block(z), at + z, b, 2 * to + c, at)

        stack(one)

    def line_relay(block, at):
        for middle, source, to in ((2, 1, 3), (1, 2, 0)):

            @pl.when(z == middle)
            def _():
                got(at + source, block(source))
                push(block(source), block(source), at + source, b, 2 * to + c, at)

    def line_got(block, at, k):
        here = (k == z) | ((z == 2) & (k == 1)) | ((z == 1) & (k == 2))

        @pl.when(jnp.logical_not(here))
        def _():
            got(at + k, block(0))

    far = lax.div(z, 2)

    def line_order(j):
        return lax.rem(z + (2, 3 - 2 * far, 1 + 2 * far, 0)[j], LINE)

    def line_add(j, rows, dst, via, at):
        to = line_order(j)
        outer_chip = (z == 0) | (z == 3)

        def direct():
            push(rows(to), dst.at[z], at + z, b, 2 * to + c, at)

        if j == 0:

            @pl.when(outer_chip)
            def _():
                push(rows(to), via, at + 4, b, 2 * (1 + far) + c, at)

            @pl.when(jnp.logical_not(outer_chip))
            def _():
                direct()

        elif j < 3:
            direct()
        else:
            keep(rows(z), dst.at[z], at + z)

    def line_via(via, at, add):
        @pl.when((z == 1) | (z == 2))
        def _():
            got(at + 4, via)
            add()

    def line_done(dst, at):
        for k in range(4):
            missing = ((z == 1) & (k == 3)) | ((z == 2) & (k == 0))

            @pl.when(jnp.logical_not(missing))
            def _():
                got(at + k, dst.at[k])

    def line_clear(dst):
        for middle, k in ((1, 3), (2, 0)):

            @pl.when(z == middle)
            def _():
                dst[k] = jnp.zeros(dst.shape[1:], BF)

    lane = lax.broadcasted_iota(jnp.int32, (1, 128), 1)
    low = lane < 64
    own24 = pl.ds(pl.multiple_of(24 * c, 8), 24)
    mate24 = pl.ds(pl.multiple_of(24 * (1 - c), 8), 24)
    part = pl.ds(pl.multiple_of(HALF * c, 128), HALF)
    chip_rows = pl.ds(pl.multiple_of(48 * chip, 16), 48)
    group_rows = pl.ds(pl.multiple_of(192 * b, 16), 192)

    barrier = pltpu.get_barrier_semaphore()

    def greet(k):
        other = lax.rem(me + k, ALL)
        pl.semaphore_signal(
            barrier, inc=1, device_id=(lax.div(other, SEQ), lax.rem(other, SEQ)), device_id_type=MESH
        )

    loop(ALL, greet, 1)

    def natural(kind, p, head):
        return kind * WIDTH + 192 * p + 64 * head

    def half_at(ref, column, high):
        tile = ref[:, column // 128 * 128 : column // 128 * 128 + 128]
        return tile if (column % 128 == 64) == high else pltpu.roll(tile, 64, 1)

    for p in range(4):
        for tile in range(5):
            pair = []
            for high in (0, 1):
                which = HALVES[2 * tile + high]
                pair.append(
                    jnp.zeros((24, 128), F32)
                    if which is None
                    else half_at(i_wqkv, natural(which[0], p, which[1]), bool(high))
                )
            r.wide_qkv[own24, 768 * p + 128 * tile : 768 * p + 128 * tile + 128] = jnp.where(
                low, pair[0], pair[1]
            )
        r.wide_qkv[own24, 768 * p + 640 : 768 * p + 768] = jnp.zeros((24, 128), F32)
    r.wide_in[own24, :] = i_win[...]
    r.wide_attn[own24, :] = i_wattn[...]
    r.w_out[z, c] = i_wout[...].astype(BF)
    r.toks[z] = i_tok[0]
    line_clear(r.r_out)
    line_clear(r.r_in)
    line_clear(r.d1r)
    for k, ref in enumerate((i_time, i_start, i_len)):
        pltpu.make_async_copy(ref, r.when.at[k], recv_sems.at[S.when + k]).start()
    for k, ref in enumerate((i_time, i_start, i_len)):
        pltpu.make_async_copy(ref, r.when.at[k], recv_sems.at[S.when + k]).wait()
    lanes8 = lax.broadcasted_iota(jnp.int32, (8, 128), 1)
    half_cond = COND // 2
    speed = jnp.exp((lanes8 % half_cond).astype(F32) * (-math.log(10000.0) / half_cond))
    angle = r.when[0, 0].astype(F32) * speed
    wave = jnp.where(lanes8 < half_cond, jnp.cos(angle), jnp.sin(angle))
    r.conds_all[b] = wave * (1.0 / (1.0 + jnp.exp(-wave)))
    pl.semaphore_wait(barrier, ALL - 1)

    def token_block(k):
        return r.toks.at[k]

    def in_block(k):
        return r.w_in.at[:, k, :, part]

    def out_block(k):
        return r.w_out.at[k, c]

    peers(lambda k, to: push(r.conds_all.at[b], r.conds_all.at[b], S.cond, to, s))
    sent(S.cond, r.conds_all.at[0:3])
    push(r.wide_qkv.at[own24], r.wide_qkv.at[own24], S.mix_qkv, b, mate)
    sent(S.mix_qkv, r.wide_qkv.at[0:24])
    push(r.wide_attn.at[own24], r.wide_attn.at[own24], S.mix_attn, b, mate)
    sent(S.mix_attn, r.wide_attn.at[0:24])
    push(r.wide_in.at[own24], r.wide_in.at[own24], S.mix_in, b, mate)
    sent(S.mix_in, r.wide_in.at[0:24])

    got(S.cond, r.conds_all.at[0:3])
    row8 = lax.broadcasted_iota(jnp.int32, (8, 128), 0)
    cond4 = jnp.zeros((8, 128), F32)
    for k in range(4):
        cond4 = jnp.where(row8 == k, r.conds_all[k], cond4)
    o_conds[...] = cond4
    wide = i_wada.shape[0]
    r.mod_pad[...] = jnp.zeros((8, 384), F32)
    r.mod_pad[:, 0:wide] = dot_nt(cond4.astype(BF), i_wada[...].astype(BF))
    columns = pltpu.roll(r.mod_pad[...], lax.rem(wide * me, 128), 1)
    for k in range(4):
        for t in range(3):
            r.mod_send[k, t : t + 1, :] = columns[k : k + 1, 128 * t : 128 * t + 128]
        r.mod_send[k, 3:4, :] = jnp.zeros((1, 128), F32)

    def send_mod(k):
        other = lax.rem(me + k, ALL)
        ob = lax.div(other, SEQ)
        push(r.mod_send.at[ob], r.mod_got.at[me], S.mod, ob, lax.rem(other, SEQ))

    loop(ALL, send_mod, 1)
    sent(S.mod, r.mod_got.at[0:31])
    keep(r.mod_send.at[b], r.mod_got.at[me], S.mod)

    def block(src, first):
        return src.at[:, pl.ds(pl.multiple_of(first, 128), HALF)]

    def along_line(src, dst, at, step):
        stack(
            lambda to: push(
                block(src, step * to + HALF * c), dst.at[chip_rows, part], at, b, 2 * to + c
            )
        )
        keep(block(src, step * z + HALF * c), dst.at[chip_rows, part], at)
        sent(at, dst.at[0:144, 0:HALF])

    def over_plane(dst, first, at):
        got(first, dst.at[0:192, 0:HALF])
        peers(
            lambda k, to: push(dst.at[group_rows, part], dst.at[group_rows, part], at, to, s)
        )
        sent(at, dst.at[0:576, 0:HALF])

    def share(dst, at, onward, rows):
        got(at, dst.at[0:rows, 0:HALF])
        push(dst.at[:, part], dst.at[:, part], onward, b, mate)
        sent(onward, dst.at[:, 0:HALF])

    got(S.mix_qkv, r.wide_qkv.at[0:24])
    r.s_qkv[...] = r.wide_qkv[...].astype(BF)
    along_line(r.s_qkv, r.w_qkv, S.w_qkv, WIDTH)
    line_gather(token_block, S.tok)
    sent(S.tok, r.toks.at[0:3])
    got(S.mix_attn, r.wide_attn.at[0:24])
    r.s_attn[...] = r.wide_attn[...].astype(BF)
    along_line(r.s_attn, r.w_attn, S.w_attn, 0)
    got(S.mix_in, r.wide_in.at[0:24])
    r.s_in[...] = r.wide_in[...].astype(BF)
    peers(
        lambda k, to: push(
            block(r.s_in, WIDTH * to + HALF * c), r.w_in.at[b, z, :, part], S.plane_in, to, s
        )
    )
    keep(block(r.s_in, WIDTH * b + HALF * c), r.w_in.at[b, z, :, part], S.plane_in)
    sent(S.plane_in, r.w_in.at[0:3, 0, :, 0:HALF])

    def start_tokens(tokens, k):
        place = (2 * k + c) * ROWS + lax.broadcasted_iota(jnp.int32, (ROWS, 1), 0)
        hidden = (place >= r.when[1, 0]) & (place < r.when[1, 0] + r.when[2, 0])
        return jnp.where(hidden, i_vec[8:9, :], tokens.astype(F32)), hidden

    x0, _ = start_tokens(i_tok[0], z)
    r.x0[...] = x0
    n1, inv1 = normalize(x0)
    r.n1[...] = n1
    r.inv1[...] = jnp.broadcast_to(inv1, (ROWS, 128))

    got(S.mod, r.mod_got)
    r.mod_flat[...] = jnp.zeros((40, 128), F32)
    for k in range(ALL):
        first = 9 * k // 8
        r.mod_flat[first : first + 3, :] += r.mod_got[k, 0:3, :]
    for k in range(6):
        row = jnp.concatenate(
            [r.mod_flat[6 * k + t : 6 * k + t + 1, :] for t in range(6)], axis=1
        )
        r.mod[k : k + 1, :] = row + i_vec[2 + k : 3 + k, :]

    def mod(k):
        return r.mod[k : k + 1, :]

    def vec(k):
        return i_vec[k : k + 1, :]

    r.h1[z] = (r.n1[...] * vec(0) * (1.0 + mod(1)) + mod(0)).astype(BF)
    r.dm[0] = (i_cot[0].astype(F32) * mod(5)).astype(BF)
    over_plane(r.w_qkv, S.w_qkv, S.group_qkv)
    peers(lambda k, to: push(r.dm.at[0], r.dm.at[k], S.dm + k, to, s))
    for k in (1, 2, 3):
        sent(S.dm + k, r.dm.at[0])

    lanes = lax.broadcasted_iota(jnp.int32, (ROWS, 128), 1)
    first_half = lanes % HD < HD // 2
    speed = jnp.exp((lanes % (HD // 2)).astype(F32) * (-math.log(10000.0) / (HD // 2)))
    row = lax.broadcasted_iota(jnp.int32, (ROWS, 128), 0)

    def table(k):
        angle = ((2 * k + c) * ROWS + row).astype(F32) * speed
        r.turn[0, k] = jnp.cos(angle)
        sine = jnp.sin(angle)
        r.turn[1, k] = jnp.where(first_half, -sine, sine)

    loop(LINE, table)

    line_relay(token_block, S.tok)

    share(r.w_qkv, S.group_qkv, S.fw_qkv, 576)
    over_plane(r.w_attn, S.w_attn, S.group_attn)
    got(S.fw_qkv, r.w_qkv.at[:, 0:HALF])

    def turned(tile, sign, k):
        other = jnp.where(first_half, pltpu.roll(tile, 96, 1), pltpu.roll(tile, 32, 1))
        return tile * r.turn[0, k] + sign * (other * r.turn[1, k])

    def project(j):
        k = lax.rem(z + j, LINE)

        @pl.when(j > 0)
        def _():
            line_got(token_block, S.tok, k)
            other, _ = start_tokens(r.toks[k], k)
            other, _ = normalize(other)
            r.h1[k] = (other * vec(0) * (1.0 + mod(1)) + mod(0)).astype(BF)

        x = dot(r.h1[k], r.w_qkv[:, 0:PACK])
        tiles = [x[:, 128 * t : 128 * t + 128] for t in range(5)]
        tiles[0] = turned(tiles[0], 1.0, k) * 0.125
        tiles[1] = jnp.where(low, turned(tiles[1], 1.0, k) * 0.125, tiles[1])
        tiles[2] = turned(tiles[2], 1.0, k)
        tiles[3] = turned(tiles[3], 1.0, k)
        for t in range(5):
            r.xb[0, k, :, 128 * t : 128 * t + 128] = tiles[t].astype(BF)
        push(r.xb.at[0, k], r.xb.at[1, k], S.xf + k, b, mate)

    loop(4, project)
    for k in range(4):
        sent(S.xf + k, r.xb.at[0, 0])

    got(S.plane_in, r.w_in.at[:, 0, :, 0:HALF])
    line_gather(in_block, S.w_in)
    sent(S.w_in, r.w_in.at[0:3, :, :, 0:HALF])
    for k in range(4):
        got(S.xf + k, r.xb.at[0, 0])

    def tile_of(t):
        return r.xb[:, :, :, 128 * t : 128 * t + 128].reshape(1024, 128)

    heads = ((0, 2, 4, True, True), (0, 2, 4, False, False), (1, 3, 1, True, False))

    def queries(head, first, size):
        q_tile, _, _, q_low, _ = heads[head]
        q = r.xb[0, first : first + size, :, 128 * q_tile : 128 * q_tile + 128]
        return jnp.where(low if q_low else ~low, q.reshape(size * 128, 128), jnp.zeros((), BF))

    for half in range(2):
        at = slice(256 * half, 256 * half + 256)
        for head in range(3):
            scores = dot_nt(tile_of(heads[head][1]), queries(head, 2 * half, 2))
            weights = jnp.exp(scores - jnp.max(scores, axis=0, keepdims=True))
            weights = weights * (1.0 / jnp.sum(weights, axis=0, keepdims=True))
            weights = weights.astype(BF)
            r.pt[head, :, at] = weights
            out = dot_tn(tile_of(heads[head][2]), weights)
            if head == 0:
                r.ot[0, 0:64, at] = out[0:64]
            elif head == 1:
                r.ot[0, 64:128, at] = out[64:128]
            else:
                r.ot[1, 0:64, at] = out[64:128]
                r.ot[1, 64:128, at] = jnp.zeros((64, 256), F32)
        for t in range(2):
            r.os[2 * half : 2 * half + 2, :, 128 * t : 128 * t + 128] = (
                r.ot[t, :, at].T.astype(BF).reshape(2, 128, 128)
            )
        for to in (2 * half, 2 * half + 1):

            @pl.when(z == to)
            def _():
                keep(r.os.at[to], r.ob.at[z], S.o)

            @pl.when(z != to)
            def _():
                push(r.os.at[to], r.ob.at[z], S.o, b, 2 * to + c)

        if half == 0:
            line_relay(in_block, S.w_in)

    sent(S.o, r.os.at[0:3])
    line_gather(out_block, S.w_out)
    sent(S.w_out, r.w_out.at[0:3, 0])
    share(r.w_attn, S.group_attn, S.fw_attn, 576)
    got(S.fw_attn, r.w_attn.at[:, 0:HALF])
    got(S.o, r.ob)
    a = jnp.zeros((ROWS, WIDTH), F32)
    for p in range(4):
        a += dot(r.ob[p, :, 0:128], r.w_attn[192 * p : 192 * p + 128, :])
        a += dot(r.ob[p, :, 128:192], r.w_attn[192 * p + 128 : 192 * p + 192, :])
    r.a[...] = a
    x1 = r.x0[...] + mod(2) * a
    r.x1[...] = x1
    n2, inv2 = normalize(x1)
    r.n2[...] = n2
    r.inv2[...] = jnp.broadcast_to(inv2, (ROWS, 128))
    r.h2[0] = (n2 * vec(1) * (1.0 + mod(4)) + mod(3)).astype(BF)
    peers(lambda k, to: push(r.h2.at[0], r.h2.at[k], S.h2 + k, to, s))
    for k in (1, 2, 3):
        sent(S.h2 + k, r.h2.at[0])
    line_relay(out_block, S.w_out)
    for k in range(4):
        line_got(in_block, S.w_in, k)
    push(r.w_in.at[:, :, :, part], r.w_in.at[:, :, :, part], S.fw_in, b, mate)
    sent(S.fw_in, r.w_in.at[:, :, :, 0:HALF])
    for k in range(4):
        line_got(out_block, S.w_out, k)
    push(r.w_out.at[:, c], r.w_out.at[:, c], S.fw_out, b, mate)
    sent(S.fw_out, r.w_out.at[:, 0])
    got(S.fw_out, r.w_out.at[:, 0])
    got(S.fw_in, r.w_in.at[:, :, :, 0:HALF])

    def feed(first, count):
        at = slice(first, first + count)
        size = count * ROWS
        u = dot(r.h2[at].reshape(size, WIDTH), r.w_in[...].reshape(WIDTH, WIDTH))
        slope = 0.7978845608028654
        cube = 0.044715
        t = jnp.tanh(slope * (u + cube * u * u * u))
        r.gb[at] = (0.5 * u * (1.0 + t)).astype(BF).reshape(count, ROWS, WIDTH)
        bend = 0.5 * (1.0 + t) + 0.5 * u * (1.0 - t * t) * (slope * (1.0 + 3.0 * cube * u * u))
        back = dot_nt(r.dm[at].reshape(size, WIDTH), r.w_out[...].reshape(WIDTH, WIDTH))
        du = (back * bend).astype(BF)
        r.du[at] = du.reshape(count, ROWS, WIDTH)
        r.dhs[at] = dot_nt(du, r.w_in[...].reshape(WIDTH, WIDTH)).astype(BF).reshape(count, ROWS, WIDTH)

    feed(0, 1)
    for first, count in ((1, 2), (3, 1)):
        for k in range(first, first + count):
            got(S.h2 + k, r.h2.at[0])
            got(S.dm + k, r.dm.at[0])
        feed(first, count)
        for k in range(first, first + count):
            push(r.dhs.at[k], r.dhr.at[k], S.dh2, near[k], s)
    sent(S.dh2, r.dhs.at[0:3])
    for t in range(3):
        at = slice(256 * t, 256 * t + 256)
        mm = dot(r.gb[...].reshape(512, WIDTH), r.w_out[:, :, :, at].reshape(WIDTH, 256))
        r.mms[:, :, at] = mm.astype(BF).reshape(4, ROWS, 256)
    peers(lambda k, to: push(r.mms.at[k], r.mmr.at[k], S.mm, to, s))
    sent(S.mm, r.mms.at[0:3])

    def gather(own, others):
        total = own[0].astype(F32)
        for k in (1, 2, 3):
            total += others[k].astype(F32)
        return total

    for k in range(2):
        rows = slice(384 * k, 384 * k + 384)
        result = dot_tn(r.gb[:, :, rows].reshape(512, 384), r.dm[...].reshape(512, 768))
        r.g_out[2 * k : 2 * k + 2] = result.astype(BF).reshape(2, 2, 96, 768)
    push(r.g_out.at[:, 1 - c], r.p_out, S.pair_out, b, mate)
    sent(S.pair_out, r.p_out)

    def outer(left, right, dst):
        for k in range(2):
            rows = slice(384 * k, 384 * k + 384)
            result = dot_tn(
                left[:, :, rows].reshape(512, 384), right[...].reshape(512, 768)
            ).astype(BF)
            dst[0, rows, :] = result[:, 0:HALF]
            dst[1, rows, :] = result[:, HALF:WIDTH]

    def to_mate(grad, dst, at):
        push(grad.at[1 - c], dst, at, b, mate)
        sent(at, dst)

    def pair_sum(grad, pair, at):
        got(at, pair)
        grad[c] = (grad[c].astype(F32) + pair[...].astype(F32)).astype(BF)

    def plane_sum(grad, dst, at):
        def rows(to):
            return grad.at[c, pl.ds(pl.multiple_of(192 * to, 16), 192)]

        peers(lambda k, to: push(rows(to), dst.at[k], at, to, s))
        keep(rows(b), dst.at[0], at)
        sent(at, dst.at[0:3])

    def line_sum(src, total, dst, first, at):
        got(first, src)
        total[...] = (
            (src[0].astype(F32) + src[1].astype(F32)) + (src[2].astype(F32) + src[3].astype(F32))
        ).astype(BF)

        def rows(to):
            return total.at[pl.ds(pl.multiple_of(48 * to, 16), 48)]

        stack(lambda to: push(rows(to), dst.at[z], at, b, 2 * to + c))
        keep(rows(z), dst.at[z], at)
        sent(at, dst.at[0:3])

    def trade(total, final, at):
        push(total.at[:, mate24], final.at[:, c], at, b, mate)
        sent(at, final.at[:, 0])
        final[:, c] = total[:, own24, :]

    for k in range(2):
        rows = slice(384 * k, 384 * k + 384)
        result = dot_tn(r.h2[:, :, rows].reshape(512, 384), r.du[...].reshape(512, 768)).astype(BF)
        for h in range(2):
            r.g_in[h, 2 * k : 2 * k + 2] = result[:, 384 * h : 384 * h + 384].reshape(2, 4, 48, 384)
    to_mate(r.g_in, r.p_in, S.pair_in)

    got(S.pair_out, r.p_out)
    for k in range(4):
        r.g_out[k, c] = (r.g_out[k, c].astype(F32) + r.p_out[k].astype(F32)).astype(BF)

    def out_rows(k):
        return r.g_out.at[k, c]

    for j in (0, 1):
        line_add(j, out_rows, r.r_out, r.via_out, S.line_out)

    def add_out():
        k = line_order(2)
        r.g_out[k, c] = (r.g_out[k, c].astype(F32) + r.via_out[...].astype(F32)).astype(BF)

    got(S.dh2, r.dhr.at[0:3])
    dh = gather(r.dhs, r.dhr)
    n2 = r.n2[...]
    inv2 = r.inv2[:, 0:1]
    r.early[...] = jnp.zeros((8, 768), F32)
    r.early[2:3, :] = jnp.sum(dh, axis=0, keepdims=True)
    both = jnp.sum(dh * n2, axis=0, keepdims=True)
    r.early[3:4, :] = both * vec(1)
    r.early[0:1, :] = both * (1.0 + mod(4))
    grad = dh * ((1.0 + mod(4)) * vec(1))
    dx1 = i_cot[0].astype(F32) + norm_back(n2, inv2, grad)
    r.dx1[...] = dx1
    r.early[1:2, :] = jnp.sum(dx1 * r.a[...], axis=0, keepdims=True)
    r.das[...] = (dx1 * mod(2)).astype(BF)
    for p in range(4):
        first = 192 * p
        r.dos[p, :, 0:128] = dot_nt(r.das[...], r.w_attn[first : first + 128, :]).astype(BF)
        tail = dot_nt(r.das[...], r.w_attn[first + 128 : first + 192, :])
        r.dos[p, :, 128:256] = jnp.concatenate(
            [tail, jnp.zeros((ROWS, 64), F32)], axis=1
        ).astype(BF)

    stack(lambda to: push(r.dos.at[to], r.dob.at[z], S.do, b, 2 * to + c))
    keep(r.dos.at[z], r.dob.at[z], S.do)
    sent(S.do, r.dos.at[0:3])

    for p in range(4):
        rows = slice(192 * p, 192 * p + 192)
        result = dot_tn(r.ob[p], r.das[...])[0:192].astype(BF)
        r.g_attn[0, rows, :] = result[:, 0:HALF]
        r.g_attn[1, rows, :] = result[:, HALF:WIDTH]
    to_mate(r.g_attn, r.p_attn, S.pair_attn)

    got(S.mm, r.mmr.at[0:3])
    mm = gather(r.mms, r.mmr)
    o_y[...] = (r.x1[...] + mod(5) * mm).astype(BF)
    r.early[4:5, :] = jnp.sum(i_cot[0].astype(F32) * mm, axis=0, keepdims=True)

    def over_line(src, dst, name):
        def one(k):
            push(src, dst.at[s], name, b, lax.rem(s + k, SEQ))

        loop(SEQ, one, 1)
        keep(src, dst.at[s], name)
        sent(name, dst.at[0:7])

    def over_group(got_ref, dst, name):
        total = got_ref[0]
        for k in range(1, SEQ):
            total += got_ref[k]
        dst[b] = total
        peers(lambda k, to: push(dst.at[b], dst.at[b], name, to, s))
        sent(name, dst.at[0:3])

    over_line(r.early, r.early_got, S.early)

    pair_sum(r.g_in, r.p_in, S.pair_in)

    line_via(r.via_out, S.line_out, add_out)
    for j in (2, 3):
        line_add(j, out_rows, r.r_out, r.via_out, S.line_out)
    sent(S.line_out, r.r_out.at[0:3])

    def in_rows(k):
        return r.g_in.at[c, :, k]

    for j in (0, 1):
        line_add(j, in_rows, r.r_in, r.via_in, S.line_in)

    def add_in():
        k = line_order(2)
        r.g_in[c, :, k] = (r.g_in[c, :, k].astype(F32) + r.via_in[...].astype(F32)).astype(BF)

    pair_sum(r.g_attn, r.p_attn, S.pair_attn)
    plane_sum(r.g_attn, r.q_attn, S.plane_attn)

    got(S.do, r.dob)
    dot0, dot1 = r.dob[:, :, 0:128].reshape(512, 128), r.dob[:, :, 128:256].reshape(512, 128)
    zero = jnp.zeros((), BF)
    moved = pltpu.roll(dot1.astype(F32), 64, 1).astype(BF)
    grads = (jnp.where(low, dot0, zero), jnp.where(low, zero, dot0), moved)
    product = dot0.astype(F32).T * r.ot[0]
    deltas = (
        jnp.sum(product[0:64], axis=0, keepdims=True),
        jnp.sum(product[64:128], axis=0, keepdims=True),
        jnp.sum(dot1.astype(F32).T * r.ot[1], axis=0, keepdims=True),
    )
    for head in range(3):
        values = tile_of(heads[head][2])
        for half in range(2):
            at = slice(256 * half, 256 * half + 256)
            dp = dot_nt(values, grads[head][at])
            r.dst[head, :, at] = (
                r.pt[head, :, at].astype(F32) * (dp - deltas[head][:, at])
            ).astype(BF)

    def key_grads(rows):
        dk = [dot(r.dst[head, rows, :], queries(head, 0, 4)) for head in range(3)]
        dv = [dot(r.pt[head, rows, :], grads[head]) for head in range(3)]
        return (dv[2], dk[0] + dk[1], dk[2], dv[0] + dv[1])

    line_via(r.via_in, S.line_in, add_in)
    for j in (2, 3):
        line_add(j, in_rows, r.r_in, r.via_in, S.line_in)
    sent(S.line_in, r.r_in.at[0:3])
    for t, tile in enumerate(key_grads(slice(512, 1024))):
        r.gps[:, 128 * t : 128 * t + 128] = tile.astype(BF)
    push(r.gps, r.gpr, S.gp, b, mate)
    sent(S.gp, r.gps)
    for t, tile in enumerate(key_grads(slice(0, 512))):
        r.ga[:, 128 * t + 128 : 128 * t + 256] = tile
    for half in range(2):
        at = slice(256 * half, 256 * half + 256)
        turned_q = [dot_tn(tile_of(heads[head][1]), r.dst[head, :, at]) for head in range(3)]
        top = jnp.concatenate([turned_q[0][0:64], turned_q[1][64:128]], axis=0)
        r.ga[at, 0:128] = top.T * 0.125
        r.ga[at, 128:256] += turned_q[2].T * 0.125
    got(S.gp, r.gpr)

    def dh1_rows(k):
        return r.d1s.at[k]

    def unproject(j):
        k = line_order(j)
        rows = pl.ds(pl.multiple_of(128 * k, 128), 128)
        tiles = [r.ga[rows, 0:128]] + [
            r.ga[rows, 128 * t : 128 * t + 128]
            + r.gpr[rows, 128 * t - 128 : 128 * t].astype(F32)
            for t in range(1, 5)
        ]
        tiles[0] = turned(tiles[0], -1.0, k)
        tiles[1] = jnp.where(low, turned(tiles[1], -1.0, k), tiles[1])
        tiles[2] = turned(tiles[2], -1.0, k)
        tiles[3] = turned(tiles[3], -1.0, k)
        for t in range(5):
            r.dqkv[k, :, 128 * t : 128 * t + 128] = tiles[t].astype(BF)
        r.dqkv[k, :, PACK:WIDTH] = jnp.zeros((128, 128), BF)
        partial_sum = dot_nt(r.dqkv[k, :, 0:PACK], r.w_qkv[:, 0:PACK])
        r.d1s[k] = partial_sum.astype(BF)
        if j == 2:

            def add():
                r.d1s[k] = (partial_sum + r.via_dh1[...].astype(F32)).astype(BF)

            line_via(r.via_dh1, S.dh1, add)
        line_add(j, dh1_rows, r.d1r, r.via_dh1, S.dh1)

    for j in range(4):
        unproject(j)
    sent(S.dh1, r.d1s.at[0:3])
    outer(r.h1, r.dqkv, r.g_qkv)
    to_mate(r.g_qkv, r.p_qkv, S.pair_qkv)
    line_sum(r.q_attn, r.m_attn, r.r_attn, S.plane_attn, S.line_attn)
    got(S.early, r.early_got)
    over_group(r.early_got, r.early_all, S.early2)
    pair_sum(r.g_qkv, r.p_qkv, S.pair_qkv)
    plane_sum(r.g_qkv, r.q_qkv, S.plane_qkv)

    line_done(r.r_in, S.line_in)
    r.m_in[...] = (
        (r.r_in[0].astype(F32) + r.r_in[1].astype(F32))
        + (r.r_in[2].astype(F32) + r.r_in[3].astype(F32))
    ).astype(BF)
    peers(lambda k, to: push(r.m_in.at[to], r.u_in.at[b], S.slice_in, to, s))
    keep(r.m_in.at[b], r.u_in.at[b], S.slice_in)
    sent(S.slice_in, r.u_in.at[0:3])
    line_sum(r.q_qkv, r.m_qkv, r.r_qkv, S.plane_qkv, S.line_qkv)

    line_done(r.d1r, S.dh1)
    dh = (r.d1r[0].astype(F32) + r.d1r[1].astype(F32)) + (
        r.d1r[2].astype(F32) + r.d1r[3].astype(F32)
    )
    n1 = r.n1[...]
    both = jnp.sum(dh * n1, axis=0, keepdims=True)
    r.late[0:1, :] = both * (1.0 + mod(1))
    r.late[1:2, :] = jnp.sum(dh, axis=0, keepdims=True)
    r.late[2:3, :] = both * vec(0)
    grad = dh * ((1.0 + mod(1)) * vec(0))
    dx0 = r.dx1[...] + norm_back(n1, r.inv1[:, 0:1], grad)
    _, hidden = start_tokens(i_tok[0], z)
    o_dx[...] = jnp.where(hidden, 0.0, dx0)
    r.late[3:4, :] = jnp.sum(jnp.where(hidden, dx0, 0.0), axis=0, keepdims=True)
    over_line(r.late, r.late_got, S.late)

    line_done(r.r_out, S.line_out)
    total = (r.r_out[0].astype(F32) + r.r_out[1].astype(F32)) + (
        r.r_out[2].astype(F32) + r.r_out[3].astype(F32)
    )
    o_gout[...] = total
    squares = total * total
    squares = jnp.sum(squares[:, 0:128] + squares[:, 128:256] + squares[:, 256:384]
                      + squares[:, 384:512] + squares[:, 512:640] + squares[:, 640:768],
                      axis=0, keepdims=True)

    def fold(value):
        total = value[:, 0:128] * value[:, 0:128]
        for t in range(1, value.shape[1] // 128):
            total += value[:, 128 * t : 128 * t + 128] * value[:, 128 * t : 128 * t + 128]
        return jnp.sum(total, axis=0, keepdims=True)

    got(S.slice_in, r.u_in)
    r.t_in[...] = r.u_in[...].astype(F32)
    trade(r.t_in, r.f_in, S.last_in)
    got(S.line_attn, r.r_attn)
    r.t_attn[0] = (r.r_attn[0].astype(F32) + r.r_attn[1].astype(F32)) + (
        r.r_attn[2].astype(F32) + r.r_attn[3].astype(F32)
    )
    trade(r.t_attn, r.f_attn, S.last_attn)
    got(S.line_qkv, r.r_qkv)
    r.t_qkv[...] = r.r_qkv[...].astype(F32)
    trade(r.t_qkv, r.f_qkv, S.last_qkv)
    got(S.late, r.late_got)
    over_group(r.late_got, r.late_all, S.late2)
    got(S.last_in, r.f_in.at[:, 0])
    got(S.last_attn, r.f_attn.at[:, 0])
    for h in range(2):
        for p in range(4):
            value = r.f_in[p, h]
            o_gin[:, 768 * p + 384 * h : 768 * p + 384 * h + 384] = value
            squares += fold(value)
        value = r.f_attn[0, h]
        o_gattn[:, 384 * h : 384 * h + 384] = value
        squares += fold(value)
    got(S.last_qkv, r.f_qkv.at[:, 0])
    where = {which: index for index, which in enumerate(HALVES) if which is not None}

    def packed_half(chunk, high):
        kind, rest = chunk // 12, chunk % 12
        index = where[(kind, rest % 3)]
        t = index // 2
        tile = r.f_qkv[rest // 3, t // 3, :, t % 3 * 128 : t % 3 * 128 + 128]
        return tile if index % 2 == high else pltpu.roll(tile, 64, 1)

    for t in range(18):
        o_gqkv[:, 128 * t : 128 * t + 128] = jnp.where(
            low, packed_half(2 * t, 0), packed_half(2 * t + 1, 1)
        )
    for p in range(4):
        for h in range(2):
            squares += fold(r.f_qkv[p, h])

    r.sq[me] = squares

    def send_sq(k):
        other = lax.rem(me + k, ALL)
        push(r.sq.at[me], r.sq.at[me], S.sq, lax.div(other, SEQ), lax.rem(other, SEQ))

    loop(ALL, send_sq, 1)
    sent(S.sq, r.sq.at[0:31])
    got(S.early2, r.early_all.at[0:3])
    got(S.late2, r.late_all.at[0:3])
    mods = []
    for k in range(4):
        early, late = r.early_all[k], r.late_all[k]
        rows = jnp.concatenate([late[1:3], early[1:5], jnp.zeros((2, 768), F32)], axis=0)
        for n in range(6):
            for m in range(6):
                r.dmod_flat[k, 6 * n + m : 6 * n + m + 1, :] = rows[
                    n : n + 1, 128 * m : 128 * m + 128
                ]
        mods.append(rows)
    gain = jnp.concatenate(
        [
            sum(r.late_all[k][0:1] for k in range(4)),
            sum(r.early_all[k][0:1] for k in range(4)),
            (mods[0] + mods[1] + mods[2] + mods[3])[0:6],
        ],
        axis=0,
    )
    mask_row = sum(r.late_all[k][3:4] for k in range(4))
    gains = jnp.concatenate([gain, mask_row, jnp.zeros((7, 768), F32)], axis=0)
    masters = jnp.concatenate([i_vec[...], jnp.zeros((7, 768), F32)], axis=0)
    own = lax.rem(WIDTH - 24 * me, WIDTH)
    o_gvec[...] = pltpu.roll(gains, own, 1)[:, 0:128]
    o_vec[...] = pltpu.roll(masters, own, 1)[:, 0:128]
    r.mod_pad[...] = jnp.zeros((8, 384), F32)
    window = lax.div(wide * me, 128)
    for k in range(4):
        rows = r.dmod_flat[k, pl.ds(window, 3), :]
        for m in range(3):
            r.mod_pad[k : k + 1, 128 * m : 128 * m + 128] = rows[m : m + 1, :]
    o_dmod[...] = pltpu.roll(r.mod_pad[...], lax.rem(384 - lax.rem(wide * me, 128), 384), 1)[:, 0:256]
    small = jnp.sum(gain * gain) + jnp.sum(mask_row * mask_row)
    conds = [r.conds_all[k][0:1].astype(BF).astype(F32) for k in range(4)]
    for k in range(4):
        for m in range(k, 4):
            term = jnp.sum(mods[k] * mods[m]) * jnp.sum(conds[k] * conds[m])
            small += term if m == k else 2.0 * term
    got(S.sq, r.sq.at[0:31])
    total = r.sq[0]
    for k in range(1, ALL):
        total += r.sq[k]
    o_norm[...] = jnp.broadcast_to(jnp.sqrt(jnp.sum(total) + small), (8, 128))

    for at, like in drains:
        left(at, like)


def run_layer(*args):
    shapes = (
        ((ROWS, WIDTH), BF),
        ((ROWS, WIDTH), F32),
        ((8, 128), F32),
        ((24, 3 * WIDTH), F32),
        ((24, WIDTH), F32),
        ((24, 4 * WIDTH), F32),
        ((96, WIDTH), F32),
        ((8, 256), F32),
        ((16, 128), F32),
        ((16, 128), F32),
        ((8, 128), F32),
    )
    whole = pl.BlockSpec(memory_space=pltpu.VMEM)
    return pl.pallas_call(
        layer_kernel,
        out_shape=[jax.ShapeDtypeStruct(shape, kind) for shape, kind in shapes],
        in_specs=[pl.BlockSpec(memory_space=pl.ANY)] * 3 + [whole] * (len(args) - 3),
        out_specs=[whole] * len(shapes),
        scratch_shapes=[pltpu.VMEM(shape, kind) for shape, kind in SCRATCH.values()]
        + [pltpu.SMEM((3, 1), jnp.int32)]
        + [pltpu.SemaphoreType.DMA((SEM_COUNT,)), pltpu.SemaphoreType.DMA((SEM_COUNT,))],
        compiler_params=pltpu.CompilerParams(
            collective_id=0, has_side_effects=True, vmem_limit_bytes=60 * 1024 * 1024
        ),
    )(*args)


def finish_kernel(
    y, dx, norm, g_qkv, g_attn, g_in, g_out, dmod, g_vec, own_vec, conds, *rest
):
    (w_ada, w_qkv, w_attn, w_in, w_out), moments, outs = rest[:5], rest[5:17], rest[17:]
    outs[0][0] = y[...]
    outs[1][0] = dx[...]
    outs[2][0, 0] = norm[0, 0]
    clip = jnp.minimum(1.0, CLIP / (norm[0:1, 0:1] + 1e-06))
    columns = w_ada.shape[0]
    rounded = conds[...].astype(BF).astype(F32)
    turned_mod = dmod[...].T
    g_ada = turned_mod[0:columns, 0:1] * rounded[0:1, :]
    for k in range(1, 4):
        g_ada += turned_mod[0:columns, k : k + 1] * rounded[k : k + 1, :]
    narrow = moments[0].shape[1]
    grads = (
        g_vec[0:9, 0:narrow],
        g_ada,
        g_qkv[...],
        g_attn[...],
        g_in[...],
        g_out[...],
    )
    weights = (
        own_vec[0:9, 0:narrow],
        w_ada[...],
        w_qkv[...],
        w_attn[...],
        w_in[...],
        w_out[...],
    )
    for k in range(6):
        results = adam_step(
            weights[k],
            grads[k] * clip,
            moments[2 * k][...],
            moments[2 * k + 1][...],
            RATE if k else RATE_VECTORS,
            DECAY if k else 0.0,
        )
        for n in range(3):
            outs[3 + 3 * k + n][...] = results[n]


def run_finish(partial_results, weights, moments):
    shapes = [((1, ROWS, WIDTH), BF), ((1, ROWS, WIDTH), F32), ((1, 1), F32)]
    for moment in moments[::2]:
        shapes += [(moment.shape, F32)] * 3
    whole = pl.BlockSpec(memory_space=pltpu.VMEM)
    specs = [whole] * len(shapes)
    specs[2] = pl.BlockSpec(memory_space=pltpu.SMEM)
    args = (*partial_results, *weights, *moments)
    return pl.pallas_call(
        finish_kernel,
        out_shape=[jax.ShapeDtypeStruct(shape, kind) for shape, kind in shapes],
        in_specs=[whole] * len(args),
        out_specs=specs,
        compiler_params=pltpu.CompilerParams(vmem_limit_bytes=60 * 1024 * 1024),
    )(*args)


def slices(
    tokens_in,
    cotangent,
    timesteps,
    span_start,
    span_len,
    vectors,
    w_ada,
    w_qkv,
    w_attn,
    w_in,
    w_out,
    m_vec,
    v_vec,
    m_ada,
    v_ada,
    m_qkv,
    v_qkv,
    m_attn,
    v_attn,
    m_in,
    v_in,
    m_out,
    v_out,
):
    partial_results = run_layer(
        timesteps,
        span_start,
        span_len,
        tokens_in,
        cotangent,
        vectors,
        w_ada.T,
        w_qkv,
        w_attn,
        w_in,
        w_out,
    )
    moments = (
        m_vec,
        v_vec,
        m_ada.T,
        v_ada.T,
        m_qkv,
        v_qkv,
        m_attn,
        v_attn,
        m_in,
        v_in,
        m_out,
        v_out,
    )
    results = run_finish(partial_results, (w_ada.T, w_qkv, w_attn, w_in, w_out), moments)
    ada_results = [result.T for result in results[6:9]]
    return (*results[:2], results[2].reshape(()), *results[3:6], *ada_results, *results[9:])


def solution(mesh):
    in_specs = (
        P("dp", "seq", None),
        P("dp", "seq", None),
        P("dp"),
        P("dp"),
        P("dp"),
        P(),
        P(None, ("dp", "seq")),
        P(("dp", "seq"), None),
        P(("dp", "seq"), None),
        P(("dp", "seq"), None),
        P(("dp", "seq"), None),
        P(None, ("dp", "seq")),
        P(None, ("dp", "seq")),
        P(None, ("dp", "seq")),
        P(None, ("dp", "seq")),
        P(("dp", "seq"), None),
        P(("dp", "seq"), None),
        P(("dp", "seq"), None),
        P(("dp", "seq"), None),
        P(("dp", "seq"), None),
        P(("dp", "seq"), None),
        P(("dp", "seq"), None),
        P(("dp", "seq"), None),
    )
    out_specs = (
        P("dp", "seq", None),
        P("dp", "seq", None),
        P(),
        P(None, ("dp", "seq")),
        P(None, ("dp", "seq")),
        P(None, ("dp", "seq")),
        P(None, ("dp", "seq")),
        P(None, ("dp", "seq")),
        P(None, ("dp", "seq")),
        P(("dp", "seq"), None),
        P(("dp", "seq"), None),
        P(("dp", "seq"), None),
        P(("dp", "seq"), None),
        P(("dp", "seq"), None),
        P(("dp", "seq"), None),
        P(("dp", "seq"), None),
        P(("dp", "seq"), None),
        P(("dp", "seq"), None),
        P(("dp", "seq"), None),
        P(("dp", "seq"), None),
        P(("dp", "seq"), None),
    )
    sizes = dict(mesh.shape)
    local = slices if (sizes["dp"], sizes["seq"]) == (4, 8) else plain
    return jax.shard_map(local, mesh=mesh, in_specs=in_specs, out_specs=out_specs, check_vma=False)
```

```python
from functools import partial
import math
from types import SimpleNamespace

import jax
import jax.numpy as jnp
from jax import lax
from jax.experimental import pallas as pl
from jax.experimental.pallas import tpu as pltpu
from jax.sharding import PartitionSpec as P

HD = 64
COND = 128
STEP = 10


BETA_ONE = 0.9
BETA_TWO = 0.999
ADAM_EPS = 1e-08
RATE = 0.1
RATE_VECTORS = 0.3
DECAY = 0.01
CLIP = 1.0
NORM_EPS = 1e-05


def cond_input(timesteps):
    half_cond = COND // 2
    freqs = jnp.exp(jnp.arange(half_cond, dtype=jnp.float32) * (-math.log(10000.0) / half_cond))
    angles = timesteps.astype(jnp.float32)[:, None] * freqs[None, :]
    return jax.nn.silu(jnp.concatenate([jnp.cos(angles), jnp.sin(angles)], axis=1))


def rotary_tables(positions):
    half_head = HD // 2
    inverse = jnp.exp(jnp.arange(half_head, dtype=jnp.float32) * (-math.log(10000.0) / half_head))
    angles = positions.astype(jnp.float32)[:, None] * inverse[None, :]
    return (jnp.cos(angles), jnp.sin(angles))


def rotate(values, cosines, sines):
    half_head = values.shape[-1] // 2
    first = values[..., :half_head]
    second = values[..., half_head:]
    cos_b = cosines[:, None, :]
    sin_b = sines[:, None, :]
    return jnp.concatenate(
        [first * cos_b - second * sin_b, second * cos_b + first * sin_b], axis=-1
    )


def rotate_back(grads, cosines, sines):
    half_head = grads.shape[-1] // 2
    first = grads[..., :half_head]
    second = grads[..., half_head:]
    cos_b = cosines[:, None, :]
    sin_b = sines[:, None, :]
    return jnp.concatenate(
        [first * cos_b + second * sin_b, second * cos_b - first * sin_b], axis=-1
    )


def normalize(values):
    centre = jnp.mean(values, axis=-1, keepdims=True)
    centred = values - centre
    inverse = lax.rsqrt(jnp.mean(centred * centred, axis=-1, keepdims=True) + NORM_EPS)
    return (centred * inverse, inverse)


def norm_back(normed, inverse, grad):
    return inverse * (
        grad
        - jnp.mean(grad, axis=-1, keepdims=True)
        - normed * jnp.mean(grad * normed, axis=-1, keepdims=True)
    )


def split_kv(block, width):
    seqs, block_rows = (block.shape[0], block.shape[1])
    keys = block[..., :width].reshape(seqs, block_rows, width // HD, HD)
    values = block[..., width:].reshape(seqs, block_rows, width // HD, HD)
    return (keys, values)


def attend_piece(carry, piece, queries, width, factor):
    piece_rows = piece.shape[1]
    size = math.gcd(piece_rows, 512)

    def attend_one_block(index, state):
        running, denom, accum = state
        block = lax.dynamic_slice_in_dim(piece, index * size, size, 1)
        keys, values = split_kv(block, width)
        scores = (
            jnp.einsum("sqhd,skhd->shqk", queries, keys, preferred_element_type=jnp.float32)
            * factor
        )
        highest = jnp.maximum(running, jnp.max(scores, axis=-1))
        shrink = jnp.exp(running - highest)
        weights = jnp.exp(scores - highest[..., None])
        denom = denom * shrink + jnp.sum(weights, axis=-1)
        accum = accum * shrink[..., None] + jnp.einsum(
            "shqk,skhd->shqd",
            weights.astype(jnp.bfloat16),
            values,
            preferred_element_type=jnp.float32,
        )
        return (highest, denom, accum)

    return lax.fori_loop(0, piece_rows // size, attend_one_block, carry)


def block_grads(block, queries, grad_out, logsum, delta, width, factor):
    keys, values = split_kv(block, width)
    scores = (
        jnp.einsum("sqhd,skhd->shqk", queries, keys, preferred_element_type=jnp.float32) * factor
    )
    probs = jnp.exp(scores - logsum[..., None])
    dprobs = jnp.einsum("sqhd,skhd->shqk", grad_out, values, preferred_element_type=jnp.float32)
    dscores = (probs * (dprobs - delta[..., None])).astype(jnp.bfloat16)
    return (keys, probs, dscores)


def query_grads(kv_all, queries, grad_out, logsum, delta, width, factor):
    total_rows = kv_all.shape[1]
    size = math.gcd(total_rows, 512)

    def query_one_block(index, accum):
        block = lax.dynamic_slice_in_dim(kv_all, index * size, size, 1)
        keys, probs, dscores = block_grads(block, queries, grad_out, logsum, delta, width, factor)
        return accum + factor * jnp.einsum(
            "shqk,skhd->sqhd", dscores, keys, preferred_element_type=jnp.float32
        )

    return lax.fori_loop(
        0, total_rows // size, query_one_block, jnp.zeros(queries.shape, jnp.float32)
    )


def key_grads(kv_all, queries, grad_out, logsum, delta, width, factor, count):
    size = math.gcd(count, 512)
    seqs = queries.shape[0]

    def key_one_block(index, accum):
        block = lax.dynamic_slice_in_dim(kv_all, index * size, size, 1)
        keys, probs, dscores = block_grads(block, queries, grad_out, logsum, delta, width, factor)
        grad_vals = jnp.einsum(
            "shqk,sqhd->skhd",
            probs.astype(jnp.bfloat16),
            grad_out,
            preferred_element_type=jnp.float32,
        )
        grad_keys = factor * jnp.einsum(
            "shqk,sqhd->skhd", dscores, queries, preferred_element_type=jnp.float32
        )
        joined = jnp.concatenate(
            [grad_keys.reshape(seqs, size, width), grad_vals.reshape(seqs, size, width)], axis=-1
        )
        return lax.dynamic_update_slice_in_dim(
            accum, jnp.transpose(joined, (1, 0, 2)), index * size, 0
        )

    initial = jnp.zeros((count, seqs, 2 * width), jnp.float32)
    return lax.fori_loop(0, count // size, key_one_block, initial)


def adam_step(weight, grad, first, second, rate, decay_rate):
    new_first = BETA_ONE * first + (1.0 - BETA_ONE) * grad
    new_second = BETA_TWO * second + (1.0 - BETA_TWO) * grad * grad
    fixed_first = new_first / (1.0 - BETA_ONE**STEP)
    fixed_second = new_second / (1.0 - BETA_TWO**STEP)
    new_weight = weight - rate * (
        fixed_first / (jnp.sqrt(fixed_second) + ADAM_EPS) + decay_rate * weight
    )
    return (new_first, new_second, new_weight)


def mod_back(grad_hidden, ln_values, normed, scale_part, gain):
    grad_shift = jnp.sum(grad_hidden, axis=1)
    grad_scale = jnp.sum(grad_hidden * ln_values, axis=1)
    grad_ln = grad_hidden * (1.0 + scale_part)
    grad_gain = jnp.sum(grad_ln * normed, axis=(0, 1))
    return (grad_shift, grad_scale, grad_gain, grad_ln * gain)


def plain(
    tokens_in,
    cotangent,
    timesteps,
    span_start,
    span_len,
    vectors,
    w_ada,
    w_qkv,
    w_attn,
    w_in,
    w_out,
    m_vec,
    v_vec,
    m_ada,
    v_ada,
    m_qkv,
    v_qkv,
    m_attn,
    v_attn,
    m_in,
    v_in,
    m_out,
    v_out,
):
    seqs, group, width = tokens_in.shape
    heads = width // HD
    factor = HD ** (-0.5)
    flat_rows = seqs * group
    full_ada, full_qkv, full_attn, full_in, full_out = (
        lax.all_gather(w_ada.astype(jnp.bfloat16), ("dp", "seq"), axis=1, tiled=True),
        lax.all_gather(w_qkv.astype(jnp.bfloat16), ("dp", "seq"), axis=0, tiled=True),
        lax.all_gather(w_attn.astype(jnp.bfloat16), ("dp", "seq"), axis=0, tiled=True),
        lax.all_gather(w_in.astype(jnp.bfloat16), ("dp", "seq"), axis=0, tiled=True),
        lax.all_gather(w_out.astype(jnp.bfloat16), ("dp", "seq"), axis=0, tiled=True),
    )
    positions = lax.axis_index("seq") * group + jnp.arange(group, dtype=jnp.int32)
    masked = (positions[None, :] >= span_start[:, None]) & (
        positions[None, :] < (span_start + span_len)[:, None]
    )
    cond_bf = cond_input(timesteps).astype(jnp.bfloat16)
    modulation = jnp.dot(cond_bf, full_ada, preferred_element_type=jnp.float32) + vectors[
        2:8
    ].reshape(1, 6 * width)
    pieces = [modulation[:, which * width : (which + 1) * width][:, None, :] for which in range(6)]
    shift_one, scale_one, gate_one, shift_two, scale_two, gate_two = pieces
    start_tokens = jnp.where(
        masked[..., None], vectors[8][None, None, :], tokens_in.astype(jnp.float32)
    )
    normed_one, inv_one = normalize(start_tokens)
    ln_one = normed_one * vectors[0]
    hidden_one = (
        (ln_one * (1.0 + scale_one) + shift_one).astype(jnp.bfloat16).reshape(flat_rows, width)
    )
    projected = jnp.dot(hidden_one, full_qkv, preferred_element_type=jnp.float32).reshape(
        seqs, group, 3 * width
    )
    cosines, sines = rotary_tables(positions)
    queries = rotate(projected[..., :width].reshape(seqs, group, heads, HD), cosines, sines).astype(
        jnp.bfloat16
    )
    keys_here = rotate(
        projected[..., width : 2 * width].reshape(seqs, group, heads, HD), cosines, sines
    ).astype(jnp.bfloat16)
    values_here = projected[..., 2 * width :].astype(jnp.bfloat16)
    kv_local = jnp.concatenate([keys_here.reshape(seqs, group, width), values_here], axis=-1)
    initial = (
        jnp.full((seqs, heads, group), -1e30, jnp.float32),
        jnp.zeros((seqs, heads, group), jnp.float32),
        jnp.zeros((seqs, heads, group, HD), jnp.float32),
    )
    running, denom, accum = attend_piece(
        initial, lax.all_gather(kv_local, "seq", axis=1, tiled=True), queries, width, factor
    )
    attn_heads = accum / denom[..., None]
    logsum = running + jnp.log(denom)
    attn_rows = jnp.transpose(attn_heads, (0, 2, 1, 3)).reshape(flat_rows, width)
    attn_bf = attn_rows.astype(jnp.bfloat16)
    branch_one = jnp.dot(attn_bf, full_attn, preferred_element_type=jnp.float32).reshape(
        seqs, group, width
    )
    mid_tokens = start_tokens + gate_one * branch_one
    normed_two, inv_two = normalize(mid_tokens)
    ln_two = normed_two * vectors[1]
    hidden_two = (
        (ln_two * (1.0 + scale_two) + shift_two).astype(jnp.bfloat16).reshape(flat_rows, width)
    )
    pre_act = jnp.dot(hidden_two, full_in, preferred_element_type=jnp.float32)
    activ, gelu_back = jax.vjp(partial(jax.nn.gelu, approximate=True), pre_act)
    activ_bf = activ.astype(jnp.bfloat16)
    branch_two = jnp.dot(activ_bf, full_out, preferred_element_type=jnp.float32).reshape(
        seqs, group, width
    )
    block_out = (mid_tokens + gate_two * branch_two).astype(jnp.bfloat16)
    grad_y = cotangent.astype(jnp.float32)
    grad_gate_two = jnp.sum(grad_y * branch_two, axis=1)
    grad_branch_two = (grad_y * gate_two).astype(jnp.bfloat16).reshape(flat_rows, width)
    grad_w_out = jnp.dot(activ_bf.T, grad_branch_two, preferred_element_type=jnp.float32)
    grad_activ = jnp.dot(grad_branch_two, full_out.T, preferred_element_type=jnp.float32)
    grad_pre = gelu_back(grad_activ)[0].astype(jnp.bfloat16)
    grad_w_in = jnp.dot(hidden_two.T, grad_pre, preferred_element_type=jnp.float32)
    grad_hidden_two = jnp.dot(grad_pre, full_in.T, preferred_element_type=jnp.float32).reshape(
        seqs, group, width
    )
    grad_shift_two, grad_scale_two, grad_gain_two, grad_normed_two = mod_back(
        grad_hidden_two, ln_two, normed_two, scale_two, vectors[1]
    )
    grad_mid = grad_y + norm_back(normed_two, inv_two, grad_normed_two)
    grad_gate_one = jnp.sum(grad_mid * branch_one, axis=1)
    grad_branch_one = (grad_mid * gate_one).astype(jnp.bfloat16).reshape(flat_rows, width)
    grad_w_attn = jnp.dot(attn_bf.T, grad_branch_one, preferred_element_type=jnp.float32)
    grad_attn_bf = (
        jnp.dot(grad_branch_one, full_attn.T, preferred_element_type=jnp.float32)
        .astype(jnp.bfloat16)
        .reshape(seqs, group, heads, HD)
    )
    delta = jnp.einsum("sqhd,shqd->shq", grad_attn_bf.astype(jnp.float32), attn_heads)
    kv_all = lax.all_gather(kv_local, "seq", axis=1, tiled=True)
    grad_queries = query_grads(kv_all, queries, grad_attn_bf, logsum, delta, width, factor)
    grad_kv = jnp.transpose(
        lax.psum_scatter(
            key_grads(
                kv_all,
                queries,
                grad_attn_bf,
                logsum,
                delta,
                width,
                factor,
                group * lax.axis_size("seq"),
            ).astype(jnp.bfloat16),
            "seq",
            scatter_dimension=0,
            tiled=True,
        ).astype(jnp.float32),
        (1, 0, 2),
    )
    grad_keys = grad_kv[..., :width].reshape(seqs, group, heads, HD)
    grad_qkv = jnp.concatenate(
        [
            rotate_back(grad_queries, cosines, sines).reshape(seqs, group, width),
            rotate_back(grad_keys, cosines, sines).reshape(seqs, group, width),
            grad_kv[..., width:],
        ],
        axis=-1,
    )
    grad_qkv = grad_qkv.astype(jnp.bfloat16).reshape(flat_rows, 3 * width)
    grad_w_qkv = jnp.dot(hidden_one.T, grad_qkv, preferred_element_type=jnp.float32)
    grad_hidden_one = jnp.dot(grad_qkv, full_qkv.T, preferred_element_type=jnp.float32).reshape(
        seqs, group, width
    )
    grad_shift_one, grad_scale_one, grad_gain_one, grad_normed_one = mod_back(
        grad_hidden_one, ln_one, normed_one, scale_one, vectors[0]
    )
    grad_start = grad_mid + norm_back(normed_one, inv_one, grad_normed_one)
    grad_mask_row = jnp.sum(jnp.where(masked[..., None], grad_start, 0.0), axis=(0, 1))
    grad_input = jnp.where(masked[..., None], 0.0, grad_start)
    grad_mod = jnp.concatenate(
        [
            grad_shift_one,
            grad_scale_one,
            grad_gate_one,
            grad_shift_two,
            grad_scale_two,
            grad_gate_two,
        ],
        axis=1,
    )
    grad_w_ada = jnp.dot(cond_bf.astype(jnp.float32).T, grad_mod, precision=lax.Precision.HIGHEST)
    grad_vectors = jnp.concatenate(
        [
            grad_gain_one[None, :],
            grad_gain_two[None, :],
            jnp.sum(grad_mod, axis=0).reshape(6, width),
            grad_mask_row[None, :],
        ],
        axis=0,
    )
    red_ada, red_qkv, red_attn, red_in, red_out, red_vec = (
        lax.psum_scatter(grad_w_ada, ("dp", "seq"), scatter_dimension=1, tiled=True),
        lax.psum_scatter(grad_w_qkv, ("dp", "seq"), scatter_dimension=0, tiled=True),
        lax.psum_scatter(grad_w_attn, ("dp", "seq"), scatter_dimension=0, tiled=True),
        lax.psum_scatter(grad_w_in, ("dp", "seq"), scatter_dimension=0, tiled=True),
        lax.psum_scatter(grad_w_out, ("dp", "seq"), scatter_dimension=0, tiled=True),
        lax.psum_scatter(grad_vectors, ("dp", "seq"), scatter_dimension=1, tiled=True),
    )
    local_squares = jnp.float32(0.0)
    for reduced in (red_vec, red_ada, red_qkv, red_attn, red_in, red_out):
        local_squares = local_squares + jnp.sum(reduced * reduced)
    grad_norm = jnp.sqrt(lax.psum(local_squares, ("dp", "seq")))
    clip_factor = jnp.minimum(1.0, CLIP / (grad_norm + 1e-06))
    columns = red_vec.shape[1]
    own_vectors = lax.dynamic_slice_in_dim(
        vectors, lax.axis_index(("dp", "seq")) * columns, columns, 1
    )
    vec_out = adam_step(own_vectors, red_vec * clip_factor, m_vec, v_vec, RATE_VECTORS, 0.0)
    ada_out = adam_step(w_ada, red_ada * clip_factor, m_ada, v_ada, RATE, DECAY)
    qkv_out = adam_step(w_qkv, red_qkv * clip_factor, m_qkv, v_qkv, RATE, DECAY)
    attn_out = adam_step(w_attn, red_attn * clip_factor, m_attn, v_attn, RATE, DECAY)
    in_out = adam_step(w_in, red_in * clip_factor, m_in, v_in, RATE, DECAY)
    out_out = adam_step(w_out, red_out * clip_factor, m_out, v_out, RATE, DECAY)
    return (
        block_out,
        grad_input,
        grad_norm,
        vec_out[0],
        vec_out[1],
        vec_out[2],
        ada_out[0],
        ada_out[1],
        ada_out[2],
        qkv_out[0],
        qkv_out[1],
        qkv_out[2],
        attn_out[0],
        attn_out[1],
        attn_out[2],
        in_out[0],
        in_out[1],
        in_out[2],
        out_out[0],
        out_out[1],
        out_out[2],
    )


F32, BF = jnp.float32, jnp.bfloat16
MESH = pl.DeviceIdType.MESH
DP, LINE, SEQ, CHIPS, ALL = 4, 4, 8, 16, 32
ROWS, WIDTH, PACK = 128, 768, 640
HALF = WIDTH // 2
HALVES = ((0, 0), (0, 1), (0, 2), (2, 2), (1, 0), (1, 1), (1, 2), None, (2, 0), (2, 1))

def numbered(**counts):
    at = {}
    for name, count in counts.items():
        at[name] = sum(counts[other] for other in at)
    return SimpleNamespace(**at), sum(counts.values())


S, SEM_COUNT = numbered(
    when=3,
    cond=1,
    mix_qkv=1,
    mix_in=1,
    mix_attn=1,
    mod=1,
    w_qkv=1,
    w_attn=1,
    plane_in=1,
    w_in=4,
    w_out=4,
    group_qkv=1,
    group_attn=1,
    fw_qkv=1,
    fw_attn=1,
    fw_in=1,
    fw_out=1,
    tok=4,
    h2=4,
    dm=4,
    xf=4,
    o=1,
    mm=1,
    dh2=1,
    do=1,
    gp=1,
    dh1=5,
    pair_out=1,
    pair_in=1,
    pair_attn=1,
    pair_qkv=1,
    plane_attn=1,
    plane_qkv=1,
    line_out=5,
    line_in=5,
    slice_in=1,
    line_attn=1,
    line_qkv=1,
    last_in=1,
    last_attn=1,
    last_qkv=1,
    early=1,
    early2=1,
    late=1,
    late2=1,
    sq=1,
)

SCRATCH = dict(
    wide_qkv=((48, 3072), F32),
    wide_in=((48, 3072), F32),
    wide_attn=((48, 768), F32),
    s_qkv=((48, 3072), BF),
    s_in=((48, 3072), BF),
    s_attn=((48, 768), BF),
    w_qkv=((768, 768), BF),
    w_in=((4, 4, 48, 768), BF),
    w_attn=((768, 768), BF),
    w_out=((4, 2, 96, 768), BF),
    conds_all=((4, 8, 128), F32),
    mod_send=((4, 4, 128), F32),
    mod_got=((32, 4, 128), F32),
    mod_flat=((40, 128), F32),
    mod_pad=((8, 384), F32),
    turn=((2, 4, 128, 128), F32),
    dmod_flat=((4, 40, 128), F32),
    mod=((8, 768), F32),
    x0=((128, 768), F32),
    n1=((128, 768), F32),
    inv1=((128, 128), F32),
    x1=((128, 768), F32),
    n2=((128, 768), F32),
    inv2=((128, 128), F32),
    a=((128, 768), F32),
    dx1=((128, 768), F32),
    toks=((4, 128, 768), BF),
    h1=((4, 128, 768), BF),
    h2=((4, 128, 768), BF),
    dm=((4, 128, 768), BF),
    gb=((4, 128, 768), BF),
    du=((4, 128, 768), BF),
    xb=((2, 4, 128, 640), BF),
    pt=((3, 1024, 512), BF),
    ot=((2, 128, 512), F32),
    os=((4, 192, 128), BF),
    ob=((4, 192, 128), BF),
    o2=((4, 128, 128), BF),
    mms=((4, 128, 768), BF),
    mmr=((4, 128, 768), BF),
    dhs=((4, 128, 768), BF),
    dhr=((4, 128, 768), BF),
    das=((128, 768), BF),
    dos=((4, 192, 128), BF),
    dob=((4, 192, 128), BF),
    dst=((3, 1024, 512), BF),
    ga=((512, 640), F32),
    gps=((512, 512), BF),
    gpr=((512, 512), BF),
    dqkv=((4, 128, 768), BF),
    d1s=((4, 128, 768), BF),
    d1r=((4, 128, 768), BF),
    g_out=((4, 2, 96, 768), BF),
    g_in=((2, 4, 4, 48, 384), BF),
    g_attn=((2, 768, 384), BF),
    g_qkv=((2, 768, 384), BF),
    p_out=((4, 96, 768), BF),
    p_in=((4, 4, 48, 384), BF),
    p_attn=((768, 384), BF),
    p_qkv=((768, 384), BF),
    q_attn=((4, 192, 384), BF),
    q_qkv=((4, 192, 384), BF),
    m_attn=((192, 384), BF),
    m_qkv=((192, 384), BF),
    r_out=((4, 96, 768), BF),
    r_in=((4, 4, 48, 384), BF),
    via_in=((4, 48, 384), BF),
    via_out=((96, 768), BF),
    via_dh1=((128, 768), BF),
    m_in=((4, 48, 384), BF),
    u_in=((4, 48, 384), BF),
    r_attn=((4, 48, 384), BF),
    r_qkv=((4, 48, 384), BF),
    t_in=((4, 48, 384), F32),
    t_attn=((1, 48, 384), F32),
    t_qkv=((4, 48, 384), F32),
    f_in=((4, 2, 24, 384), F32),
    f_attn=((1, 2, 24, 384), F32),
    f_qkv=((4, 2, 24, 384), F32),
    early=((8, 768), F32),
    early_got=((8, 8, 768), F32),
    early_all=((4, 8, 768), F32),
    late=((4, 768), F32),
    late_got=((8, 4, 768), F32),
    late_all=((4, 4, 768), F32),
    sq=((32, 1, 128), F32),
)


def dot(left, right):
    return jnp.dot(left, right, preferred_element_type=F32)


def dot_nt(left, right):
    return lax.dot_general(left, right, (((1,), (1,)), ((), ())), preferred_element_type=F32)


def dot_tn(left, right):
    return lax.dot_general(left, right, (((0,), (0,)), ((), ())), preferred_element_type=F32)


def loop(count, body, start=0):
    def step(index, carry):
        body(index)
        return carry

    lax.fori_loop(start, count, step, 0)


def layer_kernel(
    i_time,
    i_start,
    i_len,
    i_tok,
    i_cot,
    i_vec,
    i_wada,
    i_wqkv,
    i_wattn,
    i_win,
    i_wout,
    o_y,
    o_dx,
    o_norm,
    o_gqkv,
    o_gattn,
    o_gin,
    o_gout,
    o_dmod,
    o_gvec,
    o_vec,
    o_conds,
    *scratch,
):
    r = SimpleNamespace(**dict(zip(SCRATCH, scratch)), when=scratch[-3])
    send_sems, recv_sems = scratch[-2:]
    b, s = lax.axis_index("dp"), lax.axis_index("seq")
    z, c = lax.div(s, 2), lax.rem(s, 2)
    mate = s + 1 - 2 * c
    chip = b * LINE + z
    me = b * SEQ + s
    drains = []

    def push(src, dst, at, to_b, to_s, out=None):
        pltpu.make_async_remote_copy(
            src_ref=src,
            dst_ref=dst,
            send_sem=send_sems.at[at if out is None else out],
            recv_sem=recv_sems.at[at],
            device_id=(to_b, to_s),
            device_id_type=MESH,
        ).start()

    def keep(src, dst, at):
        pltpu.make_async_copy(src, dst, recv_sems.at[at]).start()

    def got(at, like):
        pltpu.make_async_copy(like, like, recv_sems.at[at]).wait()

    def left(at, like):
        pltpu.make_async_copy(like, like, send_sems.at[at]).wait()

    def sent(at, like):
        drains.append((at, like))

    near = (b, b + 1 - 2 * lax.rem(b, 2), b + 2 - 4 * lax.div(b, 2), 3 - b)

    def peers(body):
        for k in (1, 2, 3):
            body(k, near[k])

    def stack(body):
        for k in (1, 2, 3):
            body(lax.rem(z + k, LINE))

    def line_gather(block, at, near=True, rest=True):
        inner = 1 + lax.rem(z, 2)
        if near:
            push(block(z), block(z), at + z, b, 2 * inner + c, at)

        def one(to):
            relayed = ((z == 1) & (to == 3)) | ((z == 2) & (to == 0))

            @pl.when(jnp.logical_not(relayed | (to == inner)))
            def _():
                push(block(z), block(z), at + z, b, 2 * to + c, at)

        if rest:
            stack(one)

    def line_relay(block, at):
        for middle, source, to in ((2, 1, 3), (1, 2, 0)):

            @pl.when(z == middle)
            def _():
                got(at + source, block(source))
                push(block(source), block(source), at + source, b, 2 * to + c, at)

    def line_got(block, at, k):
        here = (k == z) | ((z == 2) & (k == 1)) | ((z == 1) & (k == 2))

        @pl.when(jnp.logical_not(here))
        def _():
            got(at + k, block(0))

    far = lax.div(z, 2)

    def line_order(j):
        return lax.rem(z + (2, 3 - 2 * far, 1 + 2 * far, 0)[j], LINE)

    def line_add(j, rows, dst, via, at):
        to = line_order(j)
        outer_chip = (z == 0) | (z == 3)

        def direct():
            push(rows(to), dst.at[z], at + z, b, 2 * to + c, at)

        if j == 0:

            @pl.when(outer_chip)
            def _():
                push(rows(to), via, at + 4, b, 2 * (1 + far) + c, at)

            @pl.when(jnp.logical_not(outer_chip))
            def _():
                direct()

        elif j < 3:
            direct()
        else:
            keep(rows(z), dst.at[z], at + z)

    def line_via(via, at, add):
        @pl.when((z == 1) | (z == 2))
        def _():
            got(at + 4, via)
            add()

    def line_done(dst, at):
        for k in range(4):
            missing = ((z == 1) & (k == 3)) | ((z == 2) & (k == 0))

            @pl.when(jnp.logical_not(missing))
            def _():
                got(at + k, dst.at[k])

    def line_clear(dst):
        for middle, k in ((1, 3), (2, 0)):

            @pl.when(z == middle)
            def _():
                dst[k] = jnp.zeros(dst.shape[1:], BF)

    lane = lax.broadcasted_iota(jnp.int32, (1, 128), 1)
    low = lane < 64
    own24 = pl.ds(pl.multiple_of(24 * c, 8), 24)
    mate24 = pl.ds(pl.multiple_of(24 * (1 - c), 8), 24)
    part = pl.ds(pl.multiple_of(HALF * c, 128), HALF)
    chip_rows = pl.ds(pl.multiple_of(48 * chip, 16), 48)
    group_rows = pl.ds(pl.multiple_of(192 * b, 16), 192)

    barrier = pltpu.get_barrier_semaphore()

    def greet(k):
        other = lax.rem(me + k, ALL)
        pl.semaphore_signal(
            barrier, inc=1, device_id=(lax.div(other, SEQ), lax.rem(other, SEQ)), device_id_type=MESH
        )

    loop(ALL, greet, 1)

    def natural(kind, p, head):
        return kind * WIDTH + 192 * p + 64 * head

    def half_at(ref, column, high):
        tile = ref[:, column // 128 * 128 : column // 128 * 128 + 128]
        return tile if (column % 128 == 64) == high else pltpu.roll(tile, 64, 1)

    for p in range(4):
        for tile in range(5):
            pair = []
            for high in (0, 1):
                which = HALVES[2 * tile + high]
                pair.append(
                    jnp.zeros((24, 128), F32)
                    if which is None
                    else half_at(i_wqkv, natural(which[0], p, which[1]), bool(high))
                )
            r.wide_qkv[own24, 768 * p + 128 * tile : 768 * p + 128 * tile + 128] = jnp.where(
                low, pair[0], pair[1]
            )
        r.wide_qkv[own24, 768 * p + 640 : 768 * p + 768] = jnp.zeros((24, 128), F32)
    r.wide_in[own24, :] = i_win[...]
    r.wide_attn[own24, :] = i_wattn[...]
    r.w_out[z, c] = i_wout[...].astype(BF)
    r.toks[z] = i_tok[0]
    line_clear(r.r_out)
    line_clear(r.r_in)
    line_clear(r.d1r)
    for k, ref in enumerate((i_time, i_start, i_len)):
        pltpu.make_async_copy(ref, r.when.at[k], recv_sems.at[S.when + k]).start()
    for k, ref in enumerate((i_time, i_start, i_len)):
        pltpu.make_async_copy(ref, r.when.at[k], recv_sems.at[S.when + k]).wait()
    lanes8 = lax.broadcasted_iota(jnp.int32, (8, 128), 1)
    half_cond = COND // 2
    speed = jnp.exp((lanes8 % half_cond).astype(F32) * (-math.log(10000.0) / half_cond))
    angle = r.when[0, 0].astype(F32) * speed
    wave = jnp.where(lanes8 < half_cond, jnp.cos(angle), jnp.sin(angle))
    r.conds_all[b] = wave * (1.0 / (1.0 + jnp.exp(-wave)))
    pl.semaphore_wait(barrier, ALL - 1)

    def token_block(k):
        return r.toks.at[k]

    def in_block(k):
        return r.w_in.at[:, k, :, part]

    def out_block(k):
        return r.w_out.at[k, c]

    peers(lambda k, to: push(r.conds_all.at[b], r.conds_all.at[b], S.cond, to, s))
    sent(S.cond, r.conds_all.at[0:3])
    push(r.wide_qkv.at[own24], r.wide_qkv.at[own24], S.mix_qkv, b, mate)
    sent(S.mix_qkv, r.wide_qkv.at[0:24])
    push(r.wide_attn.at[own24], r.wide_attn.at[own24], S.mix_attn, b, mate)
    sent(S.mix_attn, r.wide_attn.at[0:24])
    push(r.wide_in.at[own24], r.wide_in.at[own24], S.mix_in, b, mate)
    sent(S.mix_in, r.wide_in.at[0:24])

    got(S.cond, r.conds_all.at[0:3])
    row8 = lax.broadcasted_iota(jnp.int32, (8, 128), 0)
    cond4 = jnp.zeros((8, 128), F32)
    for k in range(4):
        cond4 = jnp.where(row8 == k, r.conds_all[k], cond4)
    o_conds[...] = cond4
    wide = i_wada.shape[0]
    r.mod_pad[...] = jnp.zeros((8, 384), F32)
    r.mod_pad[:, 0:wide] = dot_nt(cond4.astype(BF), i_wada[...].astype(BF))
    columns = pltpu.roll(r.mod_pad[...], lax.rem(wide * me, 128), 1)
    for k in range(4):
        for t in range(3):
            r.mod_send[k, t : t + 1, :] = columns[k : k + 1, 128 * t : 128 * t + 128]
        r.mod_send[k, 3:4, :] = jnp.zeros((1, 128), F32)

    def send_mod(k):
        other = lax.rem(me + k, ALL)
        ob = lax.div(other, SEQ)
        push(r.mod_send.at[ob], r.mod_got.at[me], S.mod, ob, lax.rem(other, SEQ))

    loop(ALL, send_mod, 1)
    sent(S.mod, r.mod_got.at[0:31])
    keep(r.mod_send.at[b], r.mod_got.at[me], S.mod)

    def block(src, first):
        return src.at[:, pl.ds(pl.multiple_of(first, 128), HALF)]

    def along_line(src, dst, at, step):
        stack(
            lambda to: push(
                block(src, step * to + HALF * c), dst.at[chip_rows, part], at, b, 2 * to + c
            )
        )
        keep(block(src, step * z + HALF * c), dst.at[chip_rows, part], at)
        sent(at, dst.at[0:144, 0:HALF])

    def over_plane(dst, first, at):
        got(first, dst.at[0:192, 0:HALF])
        peers(
            lambda k, to: push(dst.at[group_rows, part], dst.at[group_rows, part], at, to, s)
        )
        sent(at, dst.at[0:576, 0:HALF])

    def share(dst, at, onward, rows):
        got(at, dst.at[0:rows, 0:HALF])
        push(dst.at[:, part], dst.at[:, part], onward, b, mate)
        sent(onward, dst.at[:, 0:HALF])

    got(S.mix_qkv, r.wide_qkv.at[0:24])
    r.s_qkv[...] = r.wide_qkv[...].astype(BF)
    along_line(r.s_qkv, r.w_qkv, S.w_qkv, WIDTH)
    line_gather(token_block, S.tok, rest=False)
    sent(S.tok, r.toks.at[0:3])
    got(S.mix_attn, r.wide_attn.at[0:24])
    r.s_attn[...] = r.wide_attn[...].astype(BF)
    over_plane(r.w_qkv, S.w_qkv, S.group_qkv)
    line_gather(token_block, S.tok, near=False)
    along_line(r.s_attn, r.w_attn, S.w_attn, 0)
    got(S.mix_in, r.wide_in.at[0:24])
    r.s_in[...] = r.wide_in[...].astype(BF)
    peers(
        lambda k, to: push(
            block(r.s_in, WIDTH * to + HALF * c), r.w_in.at[b, z, :, part], S.plane_in, to, s
        )
    )
    keep(block(r.s_in, WIDTH * b + HALF * c), r.w_in.at[b, z, :, part], S.plane_in)
    sent(S.plane_in, r.w_in.at[0:3, 0, :, 0:HALF])

    def start_tokens(tokens, k):
        place = (2 * k + c) * ROWS + lax.broadcasted_iota(jnp.int32, (ROWS, 1), 0)
        hidden = (place >= r.when[1, 0]) & (place < r.when[1, 0] + r.when[2, 0])
        return jnp.where(hidden, i_vec[8:9, :], tokens.astype(F32)), hidden

    x0, _ = start_tokens(i_tok[0], z)
    r.x0[...] = x0
    n1, inv1 = normalize(x0)
    r.n1[...] = n1
    r.inv1[...] = jnp.broadcast_to(inv1, (ROWS, 128))

    got(S.mod, r.mod_got)
    r.mod_flat[...] = jnp.zeros((40, 128), F32)
    for k in range(ALL):
        first = 9 * k // 8
        r.mod_flat[first : first + 3, :] += r.mod_got[k, 0:3, :]
    for k in range(6):
        row = jnp.concatenate(
            [r.mod_flat[6 * k + t : 6 * k + t + 1, :] for t in range(6)], axis=1
        )
        r.mod[k : k + 1, :] = row + i_vec[2 + k : 3 + k, :]

    def mod(k):
        return r.mod[k : k + 1, :]

    def vec(k):
        return i_vec[k : k + 1, :]

    r.h1[z] = (r.n1[...] * vec(0) * (1.0 + mod(1)) + mod(0)).astype(BF)
    r.dm[0] = (i_cot[0].astype(F32) * mod(5)).astype(BF)
    peers(lambda k, to: push(r.dm.at[0], r.dm.at[k], S.dm + k, to, s))
    for k in (1, 2, 3):
        sent(S.dm + k, r.dm.at[0])

    lanes = lax.broadcasted_iota(jnp.int32, (ROWS, 128), 1)
    first_half = lanes % HD < HD // 2
    speed = jnp.exp((lanes % (HD // 2)).astype(F32) * (-math.log(10000.0) / (HD // 2)))
    row = lax.broadcasted_iota(jnp.int32, (ROWS, 128), 0)

    def table(k):
        angle = ((2 * k + c) * ROWS + row).astype(F32) * speed
        r.turn[0, k] = jnp.cos(angle)
        sine = jnp.sin(angle)
        r.turn[1, k] = jnp.where(first_half, -sine, sine)

    loop(LINE, table)

    line_relay(token_block, S.tok)

    share(r.w_qkv, S.group_qkv, S.fw_qkv, 576)
    over_plane(r.w_attn, S.w_attn, S.group_attn)
    got(S.fw_qkv, r.w_qkv.at[:, 0:HALF])

    def turned(tile, sign, k):
        other = jnp.where(first_half, pltpu.roll(tile, 96, 1), pltpu.roll(tile, 32, 1))
        return tile * r.turn[0, k] + sign * (other * r.turn[1, k])

    def project(j):
        k = lax.rem(z + j, LINE)

        @pl.when(j > 0)
        def _():
            line_got(token_block, S.tok, k)
            other, _ = start_tokens(r.toks[k], k)
            other, _ = normalize(other)
            r.h1[k] = (other * vec(0) * (1.0 + mod(1)) + mod(0)).astype(BF)

        x = dot(r.h1[k], r.w_qkv[:, 0:PACK])
        tiles = [x[:, 128 * t : 128 * t + 128] for t in range(5)]
        tiles[0] = turned(tiles[0], 1.0, k) * 0.125
        tiles[1] = jnp.where(low, turned(tiles[1], 1.0, k) * 0.125, tiles[1])
        tiles[2] = turned(tiles[2], 1.0, k)
        tiles[3] = turned(tiles[3], 1.0, k)
        for t in range(5):
            r.xb[0, k, :, 128 * t : 128 * t + 128] = tiles[t].astype(BF)
        push(r.xb.at[0, k], r.xb.at[1, k], S.xf + k, b, mate)

    loop(4, project)
    for k in range(4):
        sent(S.xf + k, r.xb.at[0, 0])

    got(S.plane_in, r.w_in.at[:, 0, :, 0:HALF])
    line_gather(in_block, S.w_in)
    sent(S.w_in, r.w_in.at[0:3, :, :, 0:HALF])
    for k in range(4):
        got(S.xf + k, r.xb.at[0, 0])

    def tile_of(t):
        return r.xb[:, :, :, 128 * t : 128 * t + 128].reshape(1024, 128)

    heads = ((0, 2, 4, True, True), (0, 2, 4, False, False), (1, 3, 1, True, False))

    def queries(head, first, size):
        q_tile, _, _, q_low, _ = heads[head]
        q = r.xb[0, first : first + size, :, 128 * q_tile : 128 * q_tile + 128]
        return jnp.where(low if q_low else ~low, q.reshape(size * 128, 128), jnp.zeros((), BF))

    for half in range(2):
        at = slice(256 * half, 256 * half + 256)
        for head in range(3):
            scores = dot_nt(tile_of(heads[head][1]), queries(head, 2 * half, 2))
            weights = jnp.exp(scores - jnp.max(scores, axis=0, keepdims=True))
            weights = weights * (1.0 / jnp.sum(weights, axis=0, keepdims=True))
            weights = weights.astype(BF)
            r.pt[head, :, at] = weights
            out = dot_tn(tile_of(heads[head][2]), weights)
            if head == 0:
                r.ot[0, 0:64, at] = out[0:64]
            elif head == 1:
                r.ot[0, 64:128, at] = out[64:128]
            else:
                r.ot[1, 0:64, at] = out[64:128]
                r.ot[1, 64:128, at] = jnp.zeros((64, 256), F32)
        for k in (2 * half, 2 * half + 1):
            across = slice(128 * k, 128 * k + 128)
            r.os[k, 0:128, :] = r.ot[0, :, across].T.astype(BF)
            third = r.ot[1, 0:64, across]
            third = jnp.concatenate([third, pltpu.roll(third, 64, 1)], axis=0)
            r.os[k, 128:192, :] = third.T[0:64].astype(BF)
        for to in (2 * half, 2 * half + 1):

            @pl.when(z == to)
            def _():
                keep(r.os.at[to], r.ob.at[z], S.o)

            @pl.when(z != to)
            def _():
                push(r.os.at[to], r.ob.at[z], S.o, b, 2 * to + c)

        if half == 0:
            line_relay(in_block, S.w_in)

    sent(S.o, r.os.at[0:3])
    line_gather(out_block, S.w_out)
    sent(S.w_out, r.w_out.at[0:3, 0])
    share(r.w_attn, S.group_attn, S.fw_attn, 576)
    got(S.fw_attn, r.w_attn.at[:, 0:HALF])
    got(S.o, r.ob)
    a = jnp.zeros((ROWS, WIDTH), F32)
    for p in range(4):
        third = r.ob[p, 128:192, :].astype(F32)
        third = jnp.concatenate([third, pltpu.roll(third, 64, 1)], axis=0)
        r.o2[p] = jnp.where(low, third, 0.0).astype(BF)
        a += dot(r.ob[p, 0:128, :], r.w_attn[192 * p : 192 * p + 128, :])
        a += dot(r.o2[p, :, 0:64], r.w_attn[192 * p + 128 : 192 * p + 192, :])
    r.a[...] = a
    x1 = r.x0[...] + mod(2) * a
    r.x1[...] = x1
    n2, inv2 = normalize(x1)
    r.n2[...] = n2
    r.inv2[...] = jnp.broadcast_to(inv2, (ROWS, 128))
    r.h2[0] = (n2 * vec(1) * (1.0 + mod(4)) + mod(3)).astype(BF)
    peers(lambda k, to: push(r.h2.at[0], r.h2.at[k], S.h2 + k, to, s))
    for k in (1, 2, 3):
        sent(S.h2 + k, r.h2.at[0])
    line_relay(out_block, S.w_out)
    for k in range(4):
        line_got(in_block, S.w_in, k)
    push(r.w_in.at[:, :, :, part], r.w_in.at[:, :, :, part], S.fw_in, b, mate)
    sent(S.fw_in, r.w_in.at[:, :, :, 0:HALF])
    for k in range(4):
        line_got(out_block, S.w_out, k)
    push(r.w_out.at[:, c], r.w_out.at[:, c], S.fw_out, b, mate)
    sent(S.fw_out, r.w_out.at[:, 0])
    got(S.fw_out, r.w_out.at[:, 0])
    got(S.fw_in, r.w_in.at[:, :, :, 0:HALF])

    def feed(first, count):
        at = slice(first, first + count)
        size = count * ROWS
        u = dot(r.h2[at].reshape(size, WIDTH), r.w_in[...].reshape(WIDTH, WIDTH))
        slope = 0.7978845608028654
        cube = 0.044715
        t = jnp.tanh(slope * (u + cube * u * u * u))
        r.gb[at] = (0.5 * u * (1.0 + t)).astype(BF).reshape(count, ROWS, WIDTH)
        bend = 0.5 * (1.0 + t) + 0.5 * u * (1.0 - t * t) * (slope * (1.0 + 3.0 * cube * u * u))
        back = dot_nt(r.dm[at].reshape(size, WIDTH), r.w_out[...].reshape(WIDTH, WIDTH))
        du = (back * bend).astype(BF)
        r.du[at] = du.reshape(count, ROWS, WIDTH)
        r.dhs[at] = dot_nt(du, r.w_in[...].reshape(WIDTH, WIDTH)).astype(BF).reshape(count, ROWS, WIDTH)

    feed(0, 1)
    for first, count in ((1, 2), (3, 1)):
        for k in range(first, first + count):
            got(S.h2 + k, r.h2.at[0])
            got(S.dm + k, r.dm.at[0])
        feed(first, count)
        for k in range(first, first + count):
            push(r.dhs.at[k], r.dhr.at[k], S.dh2, near[k], s)
    sent(S.dh2, r.dhs.at[0:3])
    for t in range(3):
        at = slice(256 * t, 256 * t + 256)
        mm = dot(r.gb[...].reshape(512, WIDTH), r.w_out[:, :, :, at].reshape(WIDTH, 256))
        r.mms[:, :, at] = mm.astype(BF).reshape(4, ROWS, 256)

    def gather(own, others):
        total = own[0].astype(F32)
        for k in (1, 2, 3):
            total += others[k].astype(F32)
        return total

    for k in range(2):
        rows = slice(384 * k, 384 * k + 384)
        result = dot_tn(r.gb[:, :, rows].reshape(512, 384), r.dm[...].reshape(512, 768))
        r.g_out[2 * k : 2 * k + 2] = result.astype(BF).reshape(2, 2, 96, 768)
    push(r.g_out.at[:, 1 - c], r.p_out, S.pair_out, b, mate)
    sent(S.pair_out, r.p_out)

    def outer(left, right, dst):
        for k in range(2):
            rows = slice(384 * k, 384 * k + 384)
            result = dot_tn(
                left[:, :, rows].reshape(512, 384), right[...].reshape(512, 768)
            ).astype(BF)
            dst[0, rows, :] = result[:, 0:HALF]
            dst[1, rows, :] = result[:, HALF:WIDTH]

    def to_mate(grad, dst, at):
        push(grad.at[1 - c], dst, at, b, mate)
        sent(at, dst)

    def pair_sum(grad, pair, at):
        got(at, pair)
        grad[c] = (grad[c].astype(F32) + pair[...].astype(F32)).astype(BF)

    def plane_sum(grad, dst, at):
        def rows(to):
            return grad.at[c, pl.ds(pl.multiple_of(192 * to, 16), 192)]

        peers(lambda k, to: push(rows(to), dst.at[k], at, to, s))
        keep(rows(b), dst.at[0], at)
        sent(at, dst.at[0:3])

    def line_sum(src, total, dst, first, at):
        got(first, src)
        total[...] = (
            (src[0].astype(F32) + src[1].astype(F32)) + (src[2].astype(F32) + src[3].astype(F32))
        ).astype(BF)

        def rows(to):
            return total.at[pl.ds(pl.multiple_of(48 * to, 16), 48)]

        stack(lambda to: push(rows(to), dst.at[z], at, b, 2 * to + c))
        keep(rows(z), dst.at[z], at)
        sent(at, dst.at[0:3])

    def trade(total, final, at):
        push(total.at[:, mate24], final.at[:, c], at, b, mate)
        sent(at, final.at[:, 0])
        final[:, c] = total[:, own24, :]

    for k in range(2):
        rows = slice(384 * k, 384 * k + 384)
        result = dot_tn(r.h2[:, :, rows].reshape(512, 384), r.du[...].reshape(512, 768)).astype(BF)
        for h in range(2):
            r.g_in[h, 2 * k : 2 * k + 2] = result[:, 384 * h : 384 * h + 384].reshape(2, 4, 48, 384)
    to_mate(r.g_in, r.p_in, S.pair_in)

    got(S.pair_out, r.p_out)
    for k in range(4):
        r.g_out[k, c] = (r.g_out[k, c].astype(F32) + r.p_out[k].astype(F32)).astype(BF)

    def out_rows(k):
        return r.g_out.at[k, c]

    for j in (0, 1):
        line_add(j, out_rows, r.r_out, r.via_out, S.line_out)

    def add_out():
        k = line_order(2)
        r.g_out[k, c] = (r.g_out[k, c].astype(F32) + r.via_out[...].astype(F32)).astype(BF)

    got(S.dh2, r.dhr.at[0:3])
    dh = gather(r.dhs, r.dhr)
    n2 = r.n2[...]
    inv2 = r.inv2[:, 0:1]
    r.early[...] = jnp.zeros((8, 768), F32)
    r.early[2:3, :] = jnp.sum(dh, axis=0, keepdims=True)
    both = jnp.sum(dh * n2, axis=0, keepdims=True)
    r.early[3:4, :] = both * vec(1)
    r.early[0:1, :] = both * (1.0 + mod(4))
    grad = dh * ((1.0 + mod(4)) * vec(1))
    dx1 = i_cot[0].astype(F32) + norm_back(n2, inv2, grad)
    r.dx1[...] = dx1
    r.early[1:2, :] = jnp.sum(dx1 * r.a[...], axis=0, keepdims=True)
    r.das[...] = (dx1 * mod(2)).astype(BF)
    for p in range(4):
        first = 192 * p
        r.dos[p, 0:128, :] = dot_nt(r.das[...], r.w_attn[first : first + 128, :]).astype(BF)
        tail = dot_nt(r.das[...], r.w_attn[first + 128 : first + 192, :])
        tail = jnp.concatenate([tail, jnp.zeros((ROWS, 64), F32)], axis=1)
        r.dos[p, 128:192, :] = jnp.where(low, tail[0:64], pltpu.roll(tail[64:128], 64, 1)).astype(
            BF
        )

    stack(lambda to: push(r.dos.at[to], r.dob.at[z], S.do, b, 2 * to + c))
    keep(r.dos.at[z], r.dob.at[z], S.do)
    sent(S.do, r.dos.at[0:3])
    peers(lambda k, to: push(r.mms.at[k], r.mmr.at[k], S.mm, to, s))
    sent(S.mm, r.mms.at[0:3])

    for p in range(4):
        for rows, left_side in (
            (slice(192 * p, 192 * p + 128), r.ob[p, 0:128, :]),
            (slice(192 * p + 128, 192 * p + 192), r.o2[p]),
        ):
            result = dot_tn(left_side, r.das[...])[0 : rows.stop - rows.start].astype(BF)
            r.g_attn[0, rows, :] = result[:, 0:HALF]
            r.g_attn[1, rows, :] = result[:, HALF:WIDTH]
    to_mate(r.g_attn, r.p_attn, S.pair_attn)

    def over_line(src, dst, name):
        def one(k):
            push(src, dst.at[s], name, b, lax.rem(s + k, SEQ))

        loop(SEQ, one, 1)
        keep(src, dst.at[s], name)
        sent(name, dst.at[0:7])

    def over_group(got_ref, dst, name):
        total = got_ref[0]
        for k in range(1, SEQ):
            total += got_ref[k]
        dst[b] = total
        peers(lambda k, to: push(dst.at[b], dst.at[b], name, to, s))
        sent(name, dst.at[0:3])


    pair_sum(r.g_in, r.p_in, S.pair_in)

    line_via(r.via_out, S.line_out, add_out)
    for j in (2, 3):
        line_add(j, out_rows, r.r_out, r.via_out, S.line_out)
    sent(S.line_out, r.r_out.at[0:3])

    def in_rows(k):
        return r.g_in.at[c, :, k]

    for j in (0, 1):
        line_add(j, in_rows, r.r_in, r.via_in, S.line_in)

    def add_in():
        k = line_order(2)
        r.g_in[c, :, k] = (r.g_in[c, :, k].astype(F32) + r.via_in[...].astype(F32)).astype(BF)

    pair_sum(r.g_attn, r.p_attn, S.pair_attn)
    plane_sum(r.g_attn, r.q_attn, S.plane_attn)

    got(S.do, r.dob)
    dot0 = r.dob[:, 0:128, :].reshape(512, 128)
    third = r.dob[:, 128:192, :].astype(F32).reshape(256, 128)
    other_rows = jnp.where(low, pltpu.roll(third, 64, 1), 0.0).reshape(4, 64, 128)
    third = jnp.where(low, third, 0.0).reshape(4, 64, 128)
    dot1 = jnp.concatenate([third, other_rows], axis=1).reshape(512, 128)
    zero = jnp.zeros((), BF)
    moved = pltpu.roll(dot1, 64, 1).astype(BF)
    grads = (jnp.where(low, dot0, zero), jnp.where(low, zero, dot0), moved)
    product = dot0.astype(F32).T * r.ot[0]
    deltas = (
        jnp.sum(product[0:64], axis=0, keepdims=True),
        jnp.sum(product[64:128], axis=0, keepdims=True),
        jnp.sum(dot1.T * r.ot[1], axis=0, keepdims=True),
    )
    for head in range(3):
        values = tile_of(heads[head][2])
        for half in range(2):
            at = slice(256 * half, 256 * half + 256)
            dp = dot_nt(values, grads[head][at])
            r.dst[head, :, at] = (
                r.pt[head, :, at].astype(F32) * (dp - deltas[head][:, at])
            ).astype(BF)

    def key_grads(rows):
        dk = [dot(r.dst[head, rows, :], queries(head, 0, 4)) for head in range(3)]
        dv = [dot(r.pt[head, rows, :], grads[head]) for head in range(3)]
        return (dv[2], dk[0] + dk[1], dk[2], dv[0] + dv[1])

    line_via(r.via_in, S.line_in, add_in)
    for j in (2, 3):
        line_add(j, in_rows, r.r_in, r.via_in, S.line_in)
    sent(S.line_in, r.r_in.at[0:3])
    for t, tile in enumerate(key_grads(slice(512, 1024))):
        r.gps[:, 128 * t : 128 * t + 128] = tile.astype(BF)
    push(r.gps, r.gpr, S.gp, b, mate)
    sent(S.gp, r.gps)
    for t, tile in enumerate(key_grads(slice(0, 512))):
        r.ga[:, 128 * t + 128 : 128 * t + 256] = tile
    for half in range(2):
        at = slice(256 * half, 256 * half + 256)
        turned_q = [dot_tn(tile_of(heads[head][1]), r.dst[head, :, at]) for head in range(3)]
        top = jnp.concatenate([turned_q[0][0:64], turned_q[1][64:128]], axis=0)
        r.ga[at, 0:128] = top.T * 0.125
        r.ga[at, 128:256] += turned_q[2].T * 0.125
    got(S.mm, r.mmr.at[0:3])
    mm = gather(r.mms, r.mmr)
    o_y[...] = (r.x1[...] + mod(5) * mm).astype(BF)
    r.early[4:5, :] = jnp.sum(i_cot[0].astype(F32) * mm, axis=0, keepdims=True)
    over_line(r.early, r.early_got, S.early)
    got(S.gp, r.gpr)

    def dh1_rows(k):
        return r.d1s.at[k]

    def back_turn(k):
        rows = pl.ds(pl.multiple_of(128 * k, 128), 128)
        tiles = [r.ga[rows, 0:128]] + [
            r.ga[rows, 128 * t : 128 * t + 128]
            + r.gpr[rows, 128 * t - 128 : 128 * t].astype(F32)
            for t in range(1, 5)
        ]
        tiles[0] = turned(tiles[0], -1.0, k)
        tiles[1] = jnp.where(low, turned(tiles[1], -1.0, k), tiles[1])
        tiles[2] = turned(tiles[2], -1.0, k)
        tiles[3] = turned(tiles[3], -1.0, k)
        for t in range(5):
            r.dqkv[k, :, 128 * t : 128 * t + 128] = tiles[t].astype(BF)
        r.dqkv[k, :, PACK:WIDTH] = jnp.zeros((128, 128), BF)

    loop(4, back_turn)

    def unproject(j):
        k = line_order(j)
        partial_sum = dot_nt(r.dqkv[k, :, 0:PACK], r.w_qkv[:, 0:PACK])
        r.d1s[k] = partial_sum.astype(BF)
        if j == 2:

            def add():
                r.d1s[k] = (partial_sum + r.via_dh1[...].astype(F32)).astype(BF)

            line_via(r.via_dh1, S.dh1, add)
        line_add(j, dh1_rows, r.d1r, r.via_dh1, S.dh1)

    unproject(0)
    outer(r.h1, r.dqkv, r.g_qkv)
    to_mate(r.g_qkv, r.p_qkv, S.pair_qkv)
    unproject(1)
    pair_sum(r.g_qkv, r.p_qkv, S.pair_qkv)
    plane_sum(r.g_qkv, r.q_qkv, S.plane_qkv)
    unproject(2)
    unproject(3)
    sent(S.dh1, r.d1s.at[0:3])
    line_sum(r.q_attn, r.m_attn, r.r_attn, S.plane_attn, S.line_attn)
    got(S.early, r.early_got)
    over_group(r.early_got, r.early_all, S.early2)

    line_done(r.r_in, S.line_in)
    r.m_in[...] = (
        (r.r_in[0].astype(F32) + r.r_in[1].astype(F32))
        + (r.r_in[2].astype(F32) + r.r_in[3].astype(F32))
    ).astype(BF)
    peers(lambda k, to: push(r.m_in.at[to], r.u_in.at[b], S.slice_in, to, s))
    keep(r.m_in.at[b], r.u_in.at[b], S.slice_in)
    sent(S.slice_in, r.u_in.at[0:3])
    line_sum(r.q_qkv, r.m_qkv, r.r_qkv, S.plane_qkv, S.line_qkv)

    line_done(r.d1r, S.dh1)
    dh = (r.d1r[0].astype(F32) + r.d1r[1].astype(F32)) + (
        r.d1r[2].astype(F32) + r.d1r[3].astype(F32)
    )
    n1 = r.n1[...]
    both = jnp.sum(dh * n1, axis=0, keepdims=True)
    r.late[0:1, :] = both * (1.0 + mod(1))
    r.late[1:2, :] = jnp.sum(dh, axis=0, keepdims=True)
    r.late[2:3, :] = both * vec(0)
    grad = dh * ((1.0 + mod(1)) * vec(0))
    dx0 = r.dx1[...] + norm_back(n1, r.inv1[:, 0:1], grad)
    _, hidden = start_tokens(i_tok[0], z)
    o_dx[...] = jnp.where(hidden, 0.0, dx0)
    r.late[3:4, :] = jnp.sum(jnp.where(hidden, dx0, 0.0), axis=0, keepdims=True)
    over_line(r.late, r.late_got, S.late)

    line_done(r.r_out, S.line_out)
    total = (r.r_out[0].astype(F32) + r.r_out[1].astype(F32)) + (
        r.r_out[2].astype(F32) + r.r_out[3].astype(F32)
    )
    o_gout[...] = total
    squares = total * total
    squares = jnp.sum(squares[:, 0:128] + squares[:, 128:256] + squares[:, 256:384]
                      + squares[:, 384:512] + squares[:, 512:640] + squares[:, 640:768],
                      axis=0, keepdims=True)

    def fold(value):
        total = value[:, 0:128] * value[:, 0:128]
        for t in range(1, value.shape[1] // 128):
            total += value[:, 128 * t : 128 * t + 128] * value[:, 128 * t : 128 * t + 128]
        return jnp.sum(total, axis=0, keepdims=True)

    got(S.slice_in, r.u_in)
    r.t_in[...] = r.u_in[...].astype(F32)
    trade(r.t_in, r.f_in, S.last_in)
    got(S.line_attn, r.r_attn)
    r.t_attn[0] = (r.r_attn[0].astype(F32) + r.r_attn[1].astype(F32)) + (
        r.r_attn[2].astype(F32) + r.r_attn[3].astype(F32)
    )
    trade(r.t_attn, r.f_attn, S.last_attn)
    got(S.line_qkv, r.r_qkv)
    r.t_qkv[...] = r.r_qkv[...].astype(F32)
    trade(r.t_qkv, r.f_qkv, S.last_qkv)
    got(S.late, r.late_got)
    over_group(r.late_got, r.late_all, S.late2)
    got(S.last_in, r.f_in.at[:, 0])
    got(S.last_attn, r.f_attn.at[:, 0])
    for h in range(2):
        for p in range(4):
            value = r.f_in[p, h]
            o_gin[:, 768 * p + 384 * h : 768 * p + 384 * h + 384] = value
            squares += fold(value)
        value = r.f_attn[0, h]
        o_gattn[:, 384 * h : 384 * h + 384] = value
        squares += fold(value)
    got(S.last_qkv, r.f_qkv.at[:, 0])
    where = {which: index for index, which in enumerate(HALVES) if which is not None}

    def packed_half(chunk, high):
        kind, rest = chunk // 12, chunk % 12
        index = where[(kind, rest % 3)]
        t = index // 2
        tile = r.f_qkv[rest // 3, t // 3, :, t % 3 * 128 : t % 3 * 128 + 128]
        return tile if index % 2 == high else pltpu.roll(tile, 64, 1)

    for t in range(18):
        o_gqkv[:, 128 * t : 128 * t + 128] = jnp.where(
            low, packed_half(2 * t, 0), packed_half(2 * t + 1, 1)
        )
    for p in range(4):
        for h in range(2):
            squares += fold(r.f_qkv[p, h])

    r.sq[me] = squares

    def send_sq(k):
        other = lax.rem(me + k, ALL)
        push(r.sq.at[me], r.sq.at[me], S.sq, lax.div(other, SEQ), lax.rem(other, SEQ))

    loop(ALL, send_sq, 1)
    sent(S.sq, r.sq.at[0:31])
    got(S.early2, r.early_all.at[0:3])
    got(S.late2, r.late_all.at[0:3])
    mods = []
    for k in range(4):
        early, late = r.early_all[k], r.late_all[k]
        rows = jnp.concatenate([late[1:3], early[1:5], jnp.zeros((2, 768), F32)], axis=0)
        for n in range(6):
            for m in range(6):
                r.dmod_flat[k, 6 * n + m : 6 * n + m + 1, :] = rows[
                    n : n + 1, 128 * m : 128 * m + 128
                ]
        mods.append(rows)
    gain = jnp.concatenate(
        [
            sum(r.late_all[k][0:1] for k in range(4)),
            sum(r.early_all[k][0:1] for k in range(4)),
            (mods[0] + mods[1] + mods[2] + mods[3])[0:6],
        ],
        axis=0,
    )
    mask_row = sum(r.late_all[k][3:4] for k in range(4))
    gains = jnp.concatenate([gain, mask_row, jnp.zeros((7, 768), F32)], axis=0)
    masters = jnp.concatenate([i_vec[...], jnp.zeros((7, 768), F32)], axis=0)
    own = lax.rem(WIDTH - 24 * me, WIDTH)
    o_gvec[...] = pltpu.roll(gains, own, 1)[:, 0:128]
    o_vec[...] = pltpu.roll(masters, own, 1)[:, 0:128]
    r.mod_pad[...] = jnp.zeros((8, 384), F32)
    window = lax.div(wide * me, 128)
    for k in range(4):
        rows = r.dmod_flat[k, pl.ds(window, 3), :]
        for m in range(3):
            r.mod_pad[k : k + 1, 128 * m : 128 * m + 128] = rows[m : m + 1, :]
    o_dmod[...] = pltpu.roll(r.mod_pad[...], lax.rem(384 - lax.rem(wide * me, 128), 384), 1)[:, 0:256]
    small = jnp.sum(gain * gain) + jnp.sum(mask_row * mask_row)
    conds = [r.conds_all[k][0:1].astype(BF).astype(F32) for k in range(4)]
    for k in range(4):
        for m in range(k, 4):
            term = jnp.sum(mods[k] * mods[m]) * jnp.sum(conds[k] * conds[m])
            small += term if m == k else 2.0 * term
    got(S.sq, r.sq.at[0:31])
    total = r.sq[0]
    for k in range(1, ALL):
        total += r.sq[k]
    o_norm[...] = jnp.broadcast_to(jnp.sqrt(jnp.sum(total) + small), (8, 128))

    for at, like in drains:
        left(at, like)


def run_layer(*args):
    shapes = (
        ((ROWS, WIDTH), BF),
        ((ROWS, WIDTH), F32),
        ((8, 128), F32),
        ((24, 3 * WIDTH), F32),
        ((24, WIDTH), F32),
        ((24, 4 * WIDTH), F32),
        ((96, WIDTH), F32),
        ((8, 256), F32),
        ((16, 128), F32),
        ((16, 128), F32),
        ((8, 128), F32),
    )
    whole = pl.BlockSpec(memory_space=pltpu.VMEM)
    return pl.pallas_call(
        layer_kernel,
        out_shape=[jax.ShapeDtypeStruct(shape, kind) for shape, kind in shapes],
        in_specs=[pl.BlockSpec(memory_space=pl.ANY)] * 3 + [whole] * (len(args) - 3),
        out_specs=[whole] * len(shapes),
        scratch_shapes=[pltpu.VMEM(shape, kind) for shape, kind in SCRATCH.values()]
        + [pltpu.SMEM((3, 1), jnp.int32)]
        + [pltpu.SemaphoreType.DMA((SEM_COUNT,)), pltpu.SemaphoreType.DMA((SEM_COUNT,))],
        compiler_params=pltpu.CompilerParams(
            collective_id=0, has_side_effects=True, vmem_limit_bytes=60 * 1024 * 1024
        ),
    )(*args)


def finish_kernel(
    y, dx, norm, g_qkv, g_attn, g_in, g_out, dmod, g_vec, own_vec, conds, *rest
):
    (w_ada, w_qkv, w_attn, w_in, w_out), moments, outs = rest[:5], rest[5:17], rest[17:]
    outs[0][0] = y[...]
    outs[1][0] = dx[...]
    outs[2][0, 0] = norm[0, 0]
    clip = jnp.minimum(1.0, CLIP / (norm[0:1, 0:1] + 1e-06))
    columns = w_ada.shape[0]
    rounded = conds[...].astype(BF).astype(F32)
    turned_mod = dmod[...].T
    g_ada = turned_mod[0:columns, 0:1] * rounded[0:1, :]
    for k in range(1, 4):
        g_ada += turned_mod[0:columns, k : k + 1] * rounded[k : k + 1, :]
    narrow = moments[0].shape[1]
    grads = (
        g_vec[0:9, 0:narrow],
        g_ada,
        g_qkv[...],
        g_attn[...],
        g_in[...],
        g_out[...],
    )
    weights = (
        own_vec[0:9, 0:narrow],
        w_ada[...],
        w_qkv[...],
        w_attn[...],
        w_in[...],
        w_out[...],
    )
    for k in range(6):
        results = adam_step(
            weights[k],
            grads[k] * clip,
            moments[2 * k][...],
            moments[2 * k + 1][...],
            RATE if k else RATE_VECTORS,
            DECAY if k else 0.0,
        )
        for n in range(3):
            outs[3 + 3 * k + n][...] = results[n]


def run_finish(partial_results, weights, moments):
    shapes = [((1, ROWS, WIDTH), BF), ((1, ROWS, WIDTH), F32), ((1, 1), F32)]
    for moment in moments[::2]:
        shapes += [(moment.shape, F32)] * 3
    whole = pl.BlockSpec(memory_space=pltpu.VMEM)
    specs = [whole] * len(shapes)
    specs[2] = pl.BlockSpec(memory_space=pltpu.SMEM)
    args = (*partial_results, *weights, *moments)
    return pl.pallas_call(
        finish_kernel,
        out_shape=[jax.ShapeDtypeStruct(shape, kind) for shape, kind in shapes],
        in_specs=[whole] * len(args),
        out_specs=specs,
        compiler_params=pltpu.CompilerParams(vmem_limit_bytes=60 * 1024 * 1024),
    )(*args)


def slices(
    tokens_in,
    cotangent,
    timesteps,
    span_start,
    span_len,
    vectors,
    w_ada,
    w_qkv,
    w_attn,
    w_in,
    w_out,
    m_vec,
    v_vec,
    m_ada,
    v_ada,
    m_qkv,
    v_qkv,
    m_attn,
    v_attn,
    m_in,
    v_in,
    m_out,
    v_out,
):
    partial_results = run_layer(
        timesteps,
        span_start,
        span_len,
        tokens_in,
        cotangent,
        vectors,
        w_ada.T,
        w_qkv,
        w_attn,
        w_in,
        w_out,
    )
    moments = (
        m_vec,
        v_vec,
        m_ada.T,
        v_ada.T,
        m_qkv,
        v_qkv,
        m_attn,
        v_attn,
        m_in,
        v_in,
        m_out,
        v_out,
    )
    results = run_finish(partial_results, (w_ada.T, w_qkv, w_attn, w_in, w_out), moments)
    ada_results = [result.T for result in results[6:9]]
    return (*results[:2], results[2].reshape(()), *results[3:6], *ada_results, *results[9:])


def solution(mesh):
    in_specs = (
        P("dp", "seq", None),
        P("dp", "seq", None),
        P("dp"),
        P("dp"),
        P("dp"),
        P(),
        P(None, ("dp", "seq")),
        P(("dp", "seq"), None),
        P(("dp", "seq"), None),
        P(("dp", "seq"), None),
        P(("dp", "seq"), None),
        P(None, ("dp", "seq")),
        P(None, ("dp", "seq")),
        P(None, ("dp", "seq")),
        P(None, ("dp", "seq")),
        P(("dp", "seq"), None),
        P(("dp", "seq"), None),
        P(("dp", "seq"), None),
        P(("dp", "seq"), None),
        P(("dp", "seq"), None),
        P(("dp", "seq"), None),
        P(("dp", "seq"), None),
        P(("dp", "seq"), None),
    )
    out_specs = (
        P("dp", "seq", None),
        P("dp", "seq", None),
        P(),
        P(None, ("dp", "seq")),
        P(None, ("dp", "seq")),
        P(None, ("dp", "seq")),
        P(None, ("dp", "seq")),
        P(None, ("dp", "seq")),
        P(None, ("dp", "seq")),
        P(("dp", "seq"), None),
        P(("dp", "seq"), None),
        P(("dp", "seq"), None),
        P(("dp", "seq"), None),
        P(("dp", "seq"), None),
        P(("dp", "seq"), None),
        P(("dp", "seq"), None),
        P(("dp", "seq"), None),
        P(("dp", "seq"), None),
        P(("dp", "seq"), None),
        P(("dp", "seq"), None),
        P(("dp", "seq"), None),
    )
    sizes = dict(mesh.shape)
    local = slices if (sizes["dp"], sizes["seq"]) == (4, 8) else plain
    return jax.shard_map(local, mesh=mesh, in_specs=in_specs, out_specs=out_specs, check_vma=False)
```

```python
from functools import partial
import math
from types import SimpleNamespace

import jax
import jax.numpy as jnp
from jax import lax
from jax.experimental import pallas as pl
from jax.experimental.pallas import tpu as pltpu
from jax.sharding import PartitionSpec as P

HD = 64
COND = 128
STEP = 10


BETA_ONE = 0.9
BETA_TWO = 0.999
ADAM_EPS = 1e-08
RATE = 0.1
RATE_VECTORS = 0.3
DECAY = 0.01
CLIP = 1.0
NORM_EPS = 1e-05


def cond_input(timesteps):
    half_cond = COND // 2
    freqs = jnp.exp(jnp.arange(half_cond, dtype=jnp.float32) * (-math.log(10000.0) / half_cond))
    angles = timesteps.astype(jnp.float32)[:, None] * freqs[None, :]
    return jax.nn.silu(jnp.concatenate([jnp.cos(angles), jnp.sin(angles)], axis=1))


def rotary_tables(positions):
    half_head = HD // 2
    inverse = jnp.exp(jnp.arange(half_head, dtype=jnp.float32) * (-math.log(10000.0) / half_head))
    angles = positions.astype(jnp.float32)[:, None] * inverse[None, :]
    return (jnp.cos(angles), jnp.sin(angles))


def rotate(values, cosines, sines):
    half_head = values.shape[-1] // 2
    first = values[..., :half_head]
    second = values[..., half_head:]
    cos_b = cosines[:, None, :]
    sin_b = sines[:, None, :]
    return jnp.concatenate(
        [first * cos_b - second * sin_b, second * cos_b + first * sin_b], axis=-1
    )


def rotate_back(grads, cosines, sines):
    half_head = grads.shape[-1] // 2
    first = grads[..., :half_head]
    second = grads[..., half_head:]
    cos_b = cosines[:, None, :]
    sin_b = sines[:, None, :]
    return jnp.concatenate(
        [first * cos_b + second * sin_b, second * cos_b - first * sin_b], axis=-1
    )


def normalize(values):
    centre = jnp.mean(values, axis=-1, keepdims=True)
    centred = values - centre
    inverse = lax.rsqrt(jnp.mean(centred * centred, axis=-1, keepdims=True) + NORM_EPS)
    return (centred * inverse, inverse)


def norm_back(normed, inverse, grad):
    return inverse * (
        grad
        - jnp.mean(grad, axis=-1, keepdims=True)
        - normed * jnp.mean(grad * normed, axis=-1, keepdims=True)
    )


def split_kv(block, width):
    seqs, block_rows = (block.shape[0], block.shape[1])
    keys = block[..., :width].reshape(seqs, block_rows, width // HD, HD)
    values = block[..., width:].reshape(seqs, block_rows, width // HD, HD)
    return (keys, values)


def attend_piece(carry, piece, queries, width, factor):
    piece_rows = piece.shape[1]
    size = math.gcd(piece_rows, 512)

    def attend_one_block(index, state):
        running, denom, accum = state
        block = lax.dynamic_slice_in_dim(piece, index * size, size, 1)
        keys, values = split_kv(block, width)
        scores = (
            jnp.einsum("sqhd,skhd->shqk", queries, keys, preferred_element_type=jnp.float32)
            * factor
        )
        highest = jnp.maximum(running, jnp.max(scores, axis=-1))
        shrink = jnp.exp(running - highest)
        weights = jnp.exp(scores - highest[..., None])
        denom = denom * shrink + jnp.sum(weights, axis=-1)
        accum = accum * shrink[..., None] + jnp.einsum(
            "shqk,skhd->shqd",
            weights.astype(jnp.bfloat16),
            values,
            preferred_element_type=jnp.float32,
        )
        return (highest, denom, accum)

    return lax.fori_loop(0, piece_rows // size, attend_one_block, carry)


def block_grads(block, queries, grad_out, logsum, delta, width, factor):
    keys, values = split_kv(block, width)
    scores = (
        jnp.einsum("sqhd,skhd->shqk", queries, keys, preferred_element_type=jnp.float32) * factor
    )
    probs = jnp.exp(scores - logsum[..., None])
    dprobs = jnp.einsum("sqhd,skhd->shqk", grad_out, values, preferred_element_type=jnp.float32)
    dscores = (probs * (dprobs - delta[..., None])).astype(jnp.bfloat16)
    return (keys, probs, dscores)


def query_grads(kv_all, queries, grad_out, logsum, delta, width, factor):
    total_rows = kv_all.shape[1]
    size = math.gcd(total_rows, 512)

    def query_one_block(index, accum):
        block = lax.dynamic_slice_in_dim(kv_all, index * size, size, 1)
        keys, probs, dscores = block_grads(block, queries, grad_out, logsum, delta, width, factor)
        return accum + factor * jnp.einsum(
            "shqk,skhd->sqhd", dscores, keys, preferred_element_type=jnp.float32
        )

    return lax.fori_loop(
        0, total_rows // size, query_one_block, jnp.zeros(queries.shape, jnp.float32)
    )


def key_grads(kv_all, queries, grad_out, logsum, delta, width, factor, count):
    size = math.gcd(count, 512)
    seqs = queries.shape[0]

    def key_one_block(index, accum):
        block = lax.dynamic_slice_in_dim(kv_all, index * size, size, 1)
        keys, probs, dscores = block_grads(block, queries, grad_out, logsum, delta, width, factor)
        grad_vals = jnp.einsum(
            "shqk,sqhd->skhd",
            probs.astype(jnp.bfloat16),
            grad_out,
            preferred_element_type=jnp.float32,
        )
        grad_keys = factor * jnp.einsum(
            "shqk,sqhd->skhd", dscores, queries, preferred_element_type=jnp.float32
        )
        joined = jnp.concatenate(
            [grad_keys.reshape(seqs, size, width), grad_vals.reshape(seqs, size, width)], axis=-1
        )
        return lax.dynamic_update_slice_in_dim(
            accum, jnp.transpose(joined, (1, 0, 2)), index * size, 0
        )

    initial = jnp.zeros((count, seqs, 2 * width), jnp.float32)
    return lax.fori_loop(0, count // size, key_one_block, initial)


def adam_step(weight, grad, first, second, rate, decay_rate):
    new_first = BETA_ONE * first + (1.0 - BETA_ONE) * grad
    new_second = BETA_TWO * second + (1.0 - BETA_TWO) * grad * grad
    fixed_first = new_first / (1.0 - BETA_ONE**STEP)
    fixed_second = new_second / (1.0 - BETA_TWO**STEP)
    new_weight = weight - rate * (
        fixed_first / (jnp.sqrt(fixed_second) + ADAM_EPS) + decay_rate * weight
    )
    return (new_first, new_second, new_weight)


def mod_back(grad_hidden, ln_values, normed, scale_part, gain):
    grad_shift = jnp.sum(grad_hidden, axis=1)
    grad_scale = jnp.sum(grad_hidden * ln_values, axis=1)
    grad_ln = grad_hidden * (1.0 + scale_part)
    grad_gain = jnp.sum(grad_ln * normed, axis=(0, 1))
    return (grad_shift, grad_scale, grad_gain, grad_ln * gain)


def plain(
    tokens_in,
    cotangent,
    timesteps,
    span_start,
    span_len,
    vectors,
    w_ada,
    w_qkv,
    w_attn,
    w_in,
    w_out,
    m_vec,
    v_vec,
    m_ada,
    v_ada,
    m_qkv,
    v_qkv,
    m_attn,
    v_attn,
    m_in,
    v_in,
    m_out,
    v_out,
):
    seqs, group, width = tokens_in.shape
    heads = width // HD
    factor = HD ** (-0.5)
    flat_rows = seqs * group
    full_ada, full_qkv, full_attn, full_in, full_out = (
        lax.all_gather(w_ada.astype(jnp.bfloat16), ("dp", "seq"), axis=1, tiled=True),
        lax.all_gather(w_qkv.astype(jnp.bfloat16), ("dp", "seq"), axis=0, tiled=True),
        lax.all_gather(w_attn.astype(jnp.bfloat16), ("dp", "seq"), axis=0, tiled=True),
        lax.all_gather(w_in.astype(jnp.bfloat16), ("dp", "seq"), axis=0, tiled=True),
        lax.all_gather(w_out.astype(jnp.bfloat16), ("dp", "seq"), axis=0, tiled=True),
    )
    positions = lax.axis_index("seq") * group + jnp.arange(group, dtype=jnp.int32)
    masked = (positions[None, :] >= span_start[:, None]) & (
        positions[None, :] < (span_start + span_len)[:, None]
    )
    cond_bf = cond_input(timesteps).astype(jnp.bfloat16)
    modulation = jnp.dot(cond_bf, full_ada, preferred_element_type=jnp.float32) + vectors[
        2:8
    ].reshape(1, 6 * width)
    pieces = [modulation[:, which * width : (which + 1) * width][:, None, :] for which in range(6)]
    shift_one, scale_one, gate_one, shift_two, scale_two, gate_two = pieces
    start_tokens = jnp.where(
        masked[..., None], vectors[8][None, None, :], tokens_in.astype(jnp.float32)
    )
    normed_one, inv_one = normalize(start_tokens)
    ln_one = normed_one * vectors[0]
    hidden_one = (
        (ln_one * (1.0 + scale_one) + shift_one).astype(jnp.bfloat16).reshape(flat_rows, width)
    )
    projected = jnp.dot(hidden_one, full_qkv, preferred_element_type=jnp.float32).reshape(
        seqs, group, 3 * width
    )
    cosines, sines = rotary_tables(positions)
    queries = rotate(projected[..., :width].reshape(seqs, group, heads, HD), cosines, sines).astype(
        jnp.bfloat16
    )
    keys_here = rotate(
        projected[..., width : 2 * width].reshape(seqs, group, heads, HD), cosines, sines
    ).astype(jnp.bfloat16)
    values_here = projected[..., 2 * width :].astype(jnp.bfloat16)
    kv_local = jnp.concatenate([keys_here.reshape(seqs, group, width), values_here], axis=-1)
    initial = (
        jnp.full((seqs, heads, group), -1e30, jnp.float32),
        jnp.zeros((seqs, heads, group), jnp.float32),
        jnp.zeros((seqs, heads, group, HD), jnp.float32),
    )
    running, denom, accum = attend_piece(
        initial, lax.all_gather(kv_local, "seq", axis=1, tiled=True), queries, width, factor
    )
    attn_heads = accum / denom[..., None]
    logsum = running + jnp.log(denom)
    attn_rows = jnp.transpose(attn_heads, (0, 2, 1, 3)).reshape(flat_rows, width)
    attn_bf = attn_rows.astype(jnp.bfloat16)
    branch_one = jnp.dot(attn_bf, full_attn, preferred_element_type=jnp.float32).reshape(
        seqs, group, width
    )
    mid_tokens = start_tokens + gate_one * branch_one
    normed_two, inv_two = normalize(mid_tokens)
    ln_two = normed_two * vectors[1]
    hidden_two = (
        (ln_two * (1.0 + scale_two) + shift_two).astype(jnp.bfloat16).reshape(flat_rows, width)
    )
    pre_act = jnp.dot(hidden_two, full_in, preferred_element_type=jnp.float32)
    activ, gelu_back = jax.vjp(partial(jax.nn.gelu, approximate=True), pre_act)
    activ_bf = activ.astype(jnp.bfloat16)
    branch_two = jnp.dot(activ_bf, full_out, preferred_element_type=jnp.float32).reshape(
        seqs, group, width
    )
    block_out = (mid_tokens + gate_two * branch_two).astype(jnp.bfloat16)
    grad_y = cotangent.astype(jnp.float32)
    grad_gate_two = jnp.sum(grad_y * branch_two, axis=1)
    grad_branch_two = (grad_y * gate_two).astype(jnp.bfloat16).reshape(flat_rows, width)
    grad_w_out = jnp.dot(activ_bf.T, grad_branch_two, preferred_element_type=jnp.float32)
    grad_activ = jnp.dot(grad_branch_two, full_out.T, preferred_element_type=jnp.float32)
    grad_pre = gelu_back(grad_activ)[0].astype(jnp.bfloat16)
    grad_w_in = jnp.dot(hidden_two.T, grad_pre, preferred_element_type=jnp.float32)
    grad_hidden_two = jnp.dot(grad_pre, full_in.T, preferred_element_type=jnp.float32).reshape(
        seqs, group, width
    )
    grad_shift_two, grad_scale_two, grad_gain_two, grad_normed_two = mod_back(
        grad_hidden_two, ln_two, normed_two, scale_two, vectors[1]
    )
    grad_mid = grad_y + norm_back(normed_two, inv_two, grad_normed_two)
    grad_gate_one = jnp.sum(grad_mid * branch_one, axis=1)
    grad_branch_one = (grad_mid * gate_one).astype(jnp.bfloat16).reshape(flat_rows, width)
    grad_w_attn = jnp.dot(attn_bf.T, grad_branch_one, preferred_element_type=jnp.float32)
    grad_attn_bf = (
        jnp.dot(grad_branch_one, full_attn.T, preferred_element_type=jnp.float32)
        .astype(jnp.bfloat16)
        .reshape(seqs, group, heads, HD)
    )
    delta = jnp.einsum("sqhd,shqd->shq", grad_attn_bf.astype(jnp.float32), attn_heads)
    kv_all = lax.all_gather(kv_local, "seq", axis=1, tiled=True)
    grad_queries = query_grads(kv_all, queries, grad_attn_bf, logsum, delta, width, factor)
    grad_kv = jnp.transpose(
        lax.psum_scatter(
            key_grads(
                kv_all,
                queries,
                grad_attn_bf,
                logsum,
                delta,
                width,
                factor,
                group * lax.axis_size("seq"),
            ).astype(jnp.bfloat16),
            "seq",
            scatter_dimension=0,
            tiled=True,
        ).astype(jnp.float32),
        (1, 0, 2),
    )
    grad_keys = grad_kv[..., :width].reshape(seqs, group, heads, HD)
    grad_qkv = jnp.concatenate(
        [
            rotate_back(grad_queries, cosines, sines).reshape(seqs, group, width),
            rotate_back(grad_keys, cosines, sines).reshape(seqs, group, width),
            grad_kv[..., width:],
        ],
        axis=-1,
    )
    grad_qkv = grad_qkv.astype(jnp.bfloat16).reshape(flat_rows, 3 * width)
    grad_w_qkv = jnp.dot(hidden_one.T, grad_qkv, preferred_element_type=jnp.float32)
    grad_hidden_one = jnp.dot(grad_qkv, full_qkv.T, preferred_element_type=jnp.float32).reshape(
        seqs, group, width
    )
    grad_shift_one, grad_scale_one, grad_gain_one, grad_normed_one = mod_back(
        grad_hidden_one, ln_one, normed_one, scale_one, vectors[0]
    )
    grad_start = grad_mid + norm_back(normed_one, inv_one, grad_normed_one)
    grad_mask_row = jnp.sum(jnp.where(masked[..., None], grad_start, 0.0), axis=(0, 1))
    grad_input = jnp.where(masked[..., None], 0.0, grad_start)
    grad_mod = jnp.concatenate(
        [
            grad_shift_one,
            grad_scale_one,
            grad_gate_one,
            grad_shift_two,
            grad_scale_two,
            grad_gate_two,
        ],
        axis=1,
    )
    grad_w_ada = jnp.dot(cond_bf.astype(jnp.float32).T, grad_mod, precision=lax.Precision.HIGHEST)
    grad_vectors = jnp.concatenate(
        [
            grad_gain_one[None, :],
            grad_gain_two[None, :],
            jnp.sum(grad_mod, axis=0).reshape(6, width),
            grad_mask_row[None, :],
        ],
        axis=0,
    )
    red_ada, red_qkv, red_attn, red_in, red_out, red_vec = (
        lax.psum_scatter(grad_w_ada, ("dp", "seq"), scatter_dimension=1, tiled=True),
        lax.psum_scatter(grad_w_qkv, ("dp", "seq"), scatter_dimension=0, tiled=True),
        lax.psum_scatter(grad_w_attn, ("dp", "seq"), scatter_dimension=0, tiled=True),
        lax.psum_scatter(grad_w_in, ("dp", "seq"), scatter_dimension=0, tiled=True),
        lax.psum_scatter(grad_w_out, ("dp", "seq"), scatter_dimension=0, tiled=True),
        lax.psum_scatter(grad_vectors, ("dp", "seq"), scatter_dimension=1, tiled=True),
    )
    local_squares = jnp.float32(0.0)
    for reduced in (red_vec, red_ada, red_qkv, red_attn, red_in, red_out):
        local_squares = local_squares + jnp.sum(reduced * reduced)
    grad_norm = jnp.sqrt(lax.psum(local_squares, ("dp", "seq")))
    clip_factor = jnp.minimum(1.0, CLIP / (grad_norm + 1e-06))
    columns = red_vec.shape[1]
    own_vectors = lax.dynamic_slice_in_dim(
        vectors, lax.axis_index(("dp", "seq")) * columns, columns, 1
    )
    vec_out = adam_step(own_vectors, red_vec * clip_factor, m_vec, v_vec, RATE_VECTORS, 0.0)
    ada_out = adam_step(w_ada, red_ada * clip_factor, m_ada, v_ada, RATE, DECAY)
    qkv_out = adam_step(w_qkv, red_qkv * clip_factor, m_qkv, v_qkv, RATE, DECAY)
    attn_out = adam_step(w_attn, red_attn * clip_factor, m_attn, v_attn, RATE, DECAY)
    in_out = adam_step(w_in, red_in * clip_factor, m_in, v_in, RATE, DECAY)
    out_out = adam_step(w_out, red_out * clip_factor, m_out, v_out, RATE, DECAY)
    return (
        block_out,
        grad_input,
        grad_norm,
        vec_out[0],
        vec_out[1],
        vec_out[2],
        ada_out[0],
        ada_out[1],
        ada_out[2],
        qkv_out[0],
        qkv_out[1],
        qkv_out[2],
        attn_out[0],
        attn_out[1],
        attn_out[2],
        in_out[0],
        in_out[1],
        in_out[2],
        out_out[0],
        out_out[1],
        out_out[2],
    )


F32, BF = jnp.float32, jnp.bfloat16
MESH = pl.DeviceIdType.MESH
DP, LINE, SEQ, CHIPS, ALL = 4, 4, 8, 16, 32
ROWS, WIDTH, PACK = 128, 768, 640
HALF = WIDTH // 2
HALVES = ((0, 0), (0, 1), (0, 2), (2, 2), (1, 0), (1, 1), (1, 2), None, (2, 0), (2, 1))

def numbered(**counts):
    at = {}
    for name, count in counts.items():
        at[name] = sum(counts[other] for other in at)
    return SimpleNamespace(**at), sum(counts.values())


S, SEM_COUNT = numbered(
    when=3,
    cond=1,
    mix_qkv=1,
    mix_in=1,
    mix_attn=1,
    mod=1,
    w_qkv=1,
    w_attn=1,
    plane_in=1,
    w_in=4,
    w_out=4,
    group_qkv=4,
    group_attn=4,
    fw_qkv=1,
    fw_attn=1,
    fw_in=1,
    fw_out=1,
    tok=4,
    h2=4,
    dm=4,
    xf=4,
    o=1,
    mm=1,
    dh2=1,
    do=1,
    gp=1,
    dh1=5,
    pair_out=1,
    pair_in=1,
    pair_attn=1,
    pair_qkv=1,
    plane_attn=1,
    plane_qkv=1,
    line_out=5,
    line_in=5,
    slice_in=1,
    line_attn=1,
    line_qkv=1,
    last_in=1,
    last_attn=1,
    last_qkv=1,
    early=1,
    early2=1,
    late=1,
    late2=1,
    sq=1,
)

SCRATCH = dict(
    wide_qkv=((48, 3072), F32),
    wide_in=((48, 3072), F32),
    wide_attn=((48, 768), F32),
    s_qkv=((48, 3072), BF),
    s_in=((48, 3072), BF),
    s_attn=((48, 768), BF),
    w_qkv=((768, 768), BF),
    w_in=((4, 4, 48, 768), BF),
    w_attn=((768, 768), BF),
    w_out=((4, 2, 96, 768), BF),
    conds_all=((4, 8, 128), F32),
    mod_send=((4, 4, 128), F32),
    mod_got=((32, 4, 128), F32),
    mod_flat=((40, 128), F32),
    mod_pad=((8, 384), F32),
    turn=((2, 4, 128, 128), F32),
    dmod_flat=((4, 40, 128), F32),
    mod=((8, 768), F32),
    x0=((128, 768), F32),
    n1=((128, 768), F32),
    inv1=((128, 128), F32),
    x1=((128, 768), F32),
    n2=((128, 768), F32),
    inv2=((128, 128), F32),
    a=((128, 768), F32),
    dx1=((128, 768), F32),
    toks=((4, 128, 768), BF),
    h1=((4, 128, 768), BF),
    h2=((4, 128, 768), BF),
    dm=((4, 128, 768), BF),
    gb=((4, 128, 768), BF),
    du=((4, 128, 768), BF),
    xb=((2, 4, 128, 640), BF),
    pt=((3, 1024, 512), BF),
    vt=((2, 128, 1024), BF),
    kt=((2, 128, 1024), BF),
    back=((4, 128, 768), F32),
    ot=((2, 128, 512), F32),
    os=((4, 192, 128), BF),
    ob=((4, 192, 128), BF),
    o2=((4, 128, 128), BF),
    mms=((4, 128, 768), BF),
    mmr=((4, 128, 768), BF),
    dhs=((4, 128, 768), BF),
    dhr=((4, 128, 768), BF),
    das=((128, 768), BF),
    dos=((4, 192, 128), BF),
    dob=((4, 192, 128), BF),
    dst=((3, 1024, 512), BF),
    ga=((512, 640), F32),
    gps=((512, 512), BF),
    gpr=((512, 512), BF),
    dqkv=((4, 128, 768), BF),
    d1s=((4, 128, 768), BF),
    d1r=((4, 128, 768), BF),
    g_out=((4, 2, 96, 768), BF),
    g_in=((2, 4, 4, 48, 384), BF),
    g_attn=((2, 768, 384), BF),
    g_qkv=((2, 768, 384), BF),
    p_out=((4, 96, 768), BF),
    p_in=((4, 4, 48, 384), BF),
    p_attn=((768, 384), BF),
    p_qkv=((768, 384), BF),
    q_attn=((4, 192, 384), BF),
    q_qkv=((4, 192, 384), BF),
    m_attn=((192, 384), BF),
    m_qkv=((192, 384), BF),
    r_out=((4, 96, 768), BF),
    r_in=((4, 4, 48, 384), BF),
    via_in=((4, 48, 384), BF),
    via_out=((96, 768), BF),
    via_dh1=((128, 768), BF),
    m_in=((4, 48, 384), BF),
    u_in=((4, 48, 384), BF),
    r_attn=((4, 48, 384), BF),
    r_qkv=((4, 48, 384), BF),
    t_in=((4, 48, 384), F32),
    t_attn=((1, 48, 384), F32),
    t_qkv=((4, 48, 384), F32),
    f_in=((4, 2, 24, 384), F32),
    f_attn=((1, 2, 24, 384), F32),
    f_qkv=((4, 2, 24, 384), F32),
    early=((8, 768), F32),
    early_got=((8, 8, 768), F32),
    early_all=((4, 8, 768), F32),
    late=((4, 768), F32),
    late_got=((8, 4, 768), F32),
    late_all=((4, 4, 768), F32),
    sq=((32, 1, 128), F32),
)


def dot(left, right):
    return jnp.dot(left, right, preferred_element_type=F32)


def dot_nt(left, right):
    return lax.dot_general(left, right, (((1,), (1,)), ((), ())), preferred_element_type=F32)


def dot_tn(left, right):
    return lax.dot_general(left, right, (((0,), (0,)), ((), ())), preferred_element_type=F32)


def loop(count, body, start=0):
    def step(index, carry):
        body(index)
        return carry

    lax.fori_loop(start, count, step, 0)


def layer_kernel(
    i_time,
    i_start,
    i_len,
    i_tok,
    i_cot,
    i_vec,
    i_wada,
    i_wqkv,
    i_wattn,
    i_win,
    i_wout,
    o_y,
    o_dx,
    o_norm,
    o_gqkv,
    o_gattn,
    o_gin,
    o_gout,
    o_dmod,
    o_gvec,
    o_vec,
    o_conds,
    *scratch,
):
    r = SimpleNamespace(**dict(zip(SCRATCH, scratch)), when=scratch[-3])
    send_sems, recv_sems = scratch[-2:]
    b, s = lax.axis_index("dp"), lax.axis_index("seq")
    z, c = lax.div(s, 2), lax.rem(s, 2)
    mate = s + 1 - 2 * c
    chip = b * LINE + z
    me = b * SEQ + s
    drains = []

    def push(src, dst, at, to_b, to_s, out=None):
        pltpu.make_async_remote_copy(
            src_ref=src,
            dst_ref=dst,
            send_sem=send_sems.at[at if out is None else out],
            recv_sem=recv_sems.at[at],
            device_id=(to_b, to_s),
            device_id_type=MESH,
        ).start()

    def keep(src, dst, at):
        pltpu.make_async_copy(src, dst, recv_sems.at[at]).start()

    def got(at, like):
        pltpu.make_async_copy(like, like, recv_sems.at[at]).wait()

    def left(at, like):
        pltpu.make_async_copy(like, like, send_sems.at[at]).wait()

    def sent(at, like):
        drains.append((at, like))

    near = (b, b + 1 - 2 * lax.rem(b, 2), b + 2 - 4 * lax.div(b, 2), 3 - b)

    def peers(body):
        for k in (1, 2, 3):
            body(k, near[k])

    def stack(body):
        for k in (1, 2, 3):
            body(lax.rem(z + k, LINE))

    def line_gather(block, at, near=True, rest=True):
        inner = 1 + lax.rem(z, 2)
        if near:
            push(block(z), block(z), at + z, b, 2 * inner + c, at)

        def one(to):
            relayed = ((z == 1) & (to == 3)) | ((z == 2) & (to == 0))

            @pl.when(jnp.logical_not(relayed | (to == inner)))
            def _():
                push(block(z), block(z), at + z, b, 2 * to + c, at)

        if rest:
            stack(one)

    def line_relay(block, at):
        for middle, source, to in ((2, 1, 3), (1, 2, 0)):

            @pl.when(z == middle)
            def _():
                got(at + source, block(source))
                push(block(source), block(source), at + source, b, 2 * to + c, at)

    def line_got(block, at, k):
        here = (k == z) | ((z == 2) & (k == 1)) | ((z == 1) & (k == 2))

        @pl.when(jnp.logical_not(here))
        def _():
            got(at + k, block(0))

    far = lax.div(z, 2)

    def line_order(j):
        return lax.rem(z + (2, 3 - 2 * far, 1 + 2 * far, 0)[j], LINE)

    def line_add(j, rows, dst, via, at):
        to = line_order(j)
        outer_chip = (z == 0) | (z == 3)

        def direct():
            push(rows(to), dst.at[z], at + z, b, 2 * to + c, at)

        if j == 0:

            @pl.when(outer_chip)
            def _():
                push(rows(to), via, at + 4, b, 2 * (1 + far) + c, at)

            @pl.when(jnp.logical_not(outer_chip))
            def _():
                direct()

        elif j < 3:
            direct()
        else:
            keep(rows(z), dst.at[z], at + z)

    def line_via(via, at, add):
        @pl.when((z == 1) | (z == 2))
        def _():
            got(at + 4, via)
            add()

    def line_done(dst, at):
        for k in range(4):
            missing = ((z == 1) & (k == 3)) | ((z == 2) & (k == 0))

            @pl.when(jnp.logical_not(missing))
            def _():
                got(at + k, dst.at[k])

    def line_clear(dst):
        for middle, k in ((1, 3), (2, 0)):

            @pl.when(z == middle)
            def _():
                dst[k] = jnp.zeros(dst.shape[1:], BF)

    lane = lax.broadcasted_iota(jnp.int32, (1, 128), 1)
    low = lane < 64
    own24 = pl.ds(pl.multiple_of(24 * c, 8), 24)
    mate24 = pl.ds(pl.multiple_of(24 * (1 - c), 8), 24)
    part = pl.ds(pl.multiple_of(HALF * c, 128), HALF)
    chip_rows = pl.ds(pl.multiple_of(48 * chip, 16), 48)
    group_rows = pl.ds(pl.multiple_of(192 * b, 16), 192)

    barrier = pltpu.get_barrier_semaphore()

    def greet(k):
        other = lax.rem(me + k, ALL)
        pl.semaphore_signal(
            barrier, inc=1, device_id=(lax.div(other, SEQ), lax.rem(other, SEQ)), device_id_type=MESH
        )

    loop(ALL, greet, 1)

    def natural(kind, p, head):
        return kind * WIDTH + 192 * p + 64 * head

    def half_at(ref, column, high):
        tile = ref[:, column // 128 * 128 : column // 128 * 128 + 128]
        return tile if (column % 128 == 64) == high else pltpu.roll(tile, 64, 1)

    for p in range(4):
        for tile in range(5):
            pair = []
            for high in (0, 1):
                which = HALVES[2 * tile + high]
                pair.append(
                    jnp.zeros((24, 128), F32)
                    if which is None
                    else half_at(i_wqkv, natural(which[0], p, which[1]), bool(high))
                )
            r.wide_qkv[own24, 768 * p + 128 * tile : 768 * p + 128 * tile + 128] = jnp.where(
                low, pair[0], pair[1]
            )
        r.wide_qkv[own24, 768 * p + 640 : 768 * p + 768] = jnp.zeros((24, 128), F32)
    r.wide_in[own24, :] = i_win[...]
    r.wide_attn[own24, :] = i_wattn[...]
    r.w_out[z, c] = i_wout[...].astype(BF)
    r.toks[z] = i_tok[0]
    line_clear(r.r_out)
    line_clear(r.r_in)
    line_clear(r.d1r)
    for k, ref in enumerate((i_time, i_start, i_len)):
        pltpu.make_async_copy(ref, r.when.at[k], recv_sems.at[S.when + k]).start()
    for k, ref in enumerate((i_time, i_start, i_len)):
        pltpu.make_async_copy(ref, r.when.at[k], recv_sems.at[S.when + k]).wait()
    lanes8 = lax.broadcasted_iota(jnp.int32, (8, 128), 1)
    half_cond = COND // 2
    speed = jnp.exp((lanes8 % half_cond).astype(F32) * (-math.log(10000.0) / half_cond))
    angle = r.when[0, 0].astype(F32) * speed
    wave = jnp.where(lanes8 < half_cond, jnp.cos(angle), jnp.sin(angle))
    r.conds_all[b] = wave * (1.0 / (1.0 + jnp.exp(-wave)))
    pl.semaphore_wait(barrier, ALL - 1)

    def token_block(k):
        return r.toks.at[k]

    def in_block(k):
        return r.w_in.at[:, k, :, part]

    def out_block(k):
        return r.w_out.at[k, c]

    peers(lambda k, to: push(r.conds_all.at[b], r.conds_all.at[b], S.cond, to, s))
    sent(S.cond, r.conds_all.at[0:3])
    push(r.wide_qkv.at[own24], r.wide_qkv.at[own24], S.mix_qkv, b, mate)
    sent(S.mix_qkv, r.wide_qkv.at[0:24])
    push(r.wide_attn.at[own24], r.wide_attn.at[own24], S.mix_attn, b, mate)
    sent(S.mix_attn, r.wide_attn.at[0:24])
    push(r.wide_in.at[own24], r.wide_in.at[own24], S.mix_in, b, mate)
    sent(S.mix_in, r.wide_in.at[0:24])

    got(S.cond, r.conds_all.at[0:3])
    row8 = lax.broadcasted_iota(jnp.int32, (8, 128), 0)
    cond4 = jnp.zeros((8, 128), F32)
    for k in range(4):
        cond4 = jnp.where(row8 == k, r.conds_all[k], cond4)
    o_conds[...] = cond4
    wide = i_wada.shape[0]
    r.mod_pad[...] = jnp.zeros((8, 384), F32)
    r.mod_pad[:, 0:wide] = dot_nt(cond4.astype(BF), i_wada[...].astype(BF))
    columns = pltpu.roll(r.mod_pad[...], lax.rem(wide * me, 128), 1)
    for k in range(4):
        for t in range(3):
            r.mod_send[k, t : t + 1, :] = columns[k : k + 1, 128 * t : 128 * t + 128]
        r.mod_send[k, 3:4, :] = jnp.zeros((1, 128), F32)

    def send_mod(k):
        other = lax.rem(me + k, ALL)
        ob = lax.div(other, SEQ)
        push(r.mod_send.at[ob], r.mod_got.at[me], S.mod, ob, lax.rem(other, SEQ))

    loop(ALL, send_mod, 1)
    sent(S.mod, r.mod_got.at[0:31])
    keep(r.mod_send.at[b], r.mod_got.at[me], S.mod)

    def block(src, first):
        return src.at[:, pl.ds(pl.multiple_of(first, 128), HALF)]

    def along_line(src, dst, at, step):
        stack(
            lambda to: push(
                block(src, step * to + HALF * c), dst.at[chip_rows, part], at, b, 2 * to + c
            )
        )
        keep(block(src, step * z + HALF * c), dst.at[chip_rows, part], at)
        sent(at, dst.at[0:144, 0:HALF])

    def over_plane(dst, first, at):
        got(first, dst.at[0:192, 0:HALF])
        rows = dst.at[group_rows, part]
        for k in (1, 2, 3):
            push(rows, rows, at + k, near[k], s)
            sent(at + k, dst.at[0:192, 0:HALF])

    def share(dst, at, onward):
        for k in range(4):
            rows = dst.at[pl.ds(pl.multiple_of(192 * near[k], 16), 192), part]
            if k:
                got(at + k, rows)
            push(rows, rows, onward, b, mate)
        sent(onward, dst.at[:, 0:HALF])

    def line_share(block, at, onward):
        for k in range(4):
            line_got(block, at, k)
            push(block(k), block(k), onward, b, mate)

    got(S.mix_qkv, r.wide_qkv.at[0:24])
    r.s_qkv[...] = r.wide_qkv[...].astype(BF)
    along_line(r.s_qkv, r.w_qkv, S.w_qkv, WIDTH)
    line_gather(token_block, S.tok, rest=False)
    sent(S.tok, r.toks.at[0:3])
    got(S.mix_attn, r.wide_attn.at[0:24])
    r.s_attn[...] = r.wide_attn[...].astype(BF)
    over_plane(r.w_qkv, S.w_qkv, S.group_qkv)
    line_gather(token_block, S.tok, near=False)
    along_line(r.s_attn, r.w_attn, S.w_attn, 0)
    line_gather(out_block, S.w_out)
    sent(S.w_out, r.w_out.at[0:3, 0])
    got(S.mix_in, r.wide_in.at[0:24])
    r.s_in[...] = r.wide_in[...].astype(BF)
    peers(
        lambda k, to: push(
            block(r.s_in, WIDTH * to + HALF * c), r.w_in.at[b, z, :, part], S.plane_in, to, s
        )
    )
    keep(block(r.s_in, WIDTH * b + HALF * c), r.w_in.at[b, z, :, part], S.plane_in)
    sent(S.plane_in, r.w_in.at[0:3, 0, :, 0:HALF])

    def start_tokens(tokens, k):
        place = (2 * k + c) * ROWS + lax.broadcasted_iota(jnp.int32, (ROWS, 1), 0)
        hidden = (place >= r.when[1, 0]) & (place < r.when[1, 0] + r.when[2, 0])
        return jnp.where(hidden, i_vec[8:9, :], tokens.astype(F32)), hidden

    x0, _ = start_tokens(i_tok[0], z)
    r.x0[...] = x0
    n1, inv1 = normalize(x0)
    r.n1[...] = n1
    r.inv1[...] = jnp.broadcast_to(inv1, (ROWS, 128))

    got(S.mod, r.mod_got)
    r.mod_flat[...] = jnp.zeros((40, 128), F32)
    for k in range(ALL):
        first = 9 * k // 8
        r.mod_flat[first : first + 3, :] += r.mod_got[k, 0:3, :]
    for k in range(6):
        row = jnp.concatenate(
            [r.mod_flat[6 * k + t : 6 * k + t + 1, :] for t in range(6)], axis=1
        )
        r.mod[k : k + 1, :] = row + i_vec[2 + k : 3 + k, :]

    def mod(k):
        return r.mod[k : k + 1, :]

    def vec(k):
        return i_vec[k : k + 1, :]

    r.h1[z] = (r.n1[...] * vec(0) * (1.0 + mod(1)) + mod(0)).astype(BF)
    r.dm[0] = (i_cot[0].astype(F32) * mod(5)).astype(BF)
    peers(lambda k, to: push(r.dm.at[0], r.dm.at[k], S.dm + k, to, s))
    for k in (1, 2, 3):
        sent(S.dm + k, r.dm.at[0])

    lanes = lax.broadcasted_iota(jnp.int32, (ROWS, 128), 1)
    first_half = lanes % HD < HD // 2
    speed = jnp.exp((lanes % (HD // 2)).astype(F32) * (-math.log(10000.0) / (HD // 2)))
    row = lax.broadcasted_iota(jnp.int32, (ROWS, 128), 0)

    def table(k):
        angle = ((2 * k + c) * ROWS + row).astype(F32) * speed
        r.turn[0, k] = jnp.cos(angle)
        sine = jnp.sin(angle)
        r.turn[1, k] = jnp.where(first_half, -sine, sine)

    loop(LINE, table)

    line_relay(token_block, S.tok)

    share(r.w_qkv, S.group_qkv, S.fw_qkv)
    over_plane(r.w_attn, S.w_attn, S.group_attn)
    got(S.fw_qkv, r.w_qkv.at[:, 0:HALF])

    def turned(tile, sign, k):
        other = jnp.where(first_half, pltpu.roll(tile, 96, 1), pltpu.roll(tile, 32, 1))
        return tile * r.turn[0, k] + sign * (other * r.turn[1, k])

    def project(j):
        k = lax.rem(z + j, LINE)

        @pl.when(j > 0)
        def _():
            line_got(token_block, S.tok, k)
            other, _ = start_tokens(r.toks[k], k)
            other, _ = normalize(other)
            r.h1[k] = (other * vec(0) * (1.0 + mod(1)) + mod(0)).astype(BF)

        x = dot(r.h1[k], r.w_qkv[:, 0:PACK])
        tiles = [x[:, 128 * t : 128 * t + 128] for t in range(5)]
        tiles[0] = turned(tiles[0], 1.0, k) * 0.125
        tiles[1] = jnp.where(low, turned(tiles[1], 1.0, k) * 0.125, tiles[1])
        tiles[2] = turned(tiles[2], 1.0, k)
        tiles[3] = turned(tiles[3], 1.0, k)
        for t in range(5):
            r.xb[0, k, :, 128 * t : 128 * t + 128] = tiles[t].astype(BF)
        push(r.xb.at[0, k], r.xb.at[1, k], S.xf + k, b, mate)

    loop(4, project)
    for k in range(4):
        sent(S.xf + k, r.xb.at[0, 0])

    for k in range(4):
        got(S.xf + k, r.xb.at[0, 0])

    def tile_of(t):
        return r.xb[:, :, :, 128 * t : 128 * t + 128].reshape(1024, 128)

    heads = ((0, 2, 4, True, True), (0, 2, 4, False, False), (1, 3, 1, True, False))

    def queries(head, first, size):
        q_tile, _, _, q_low, _ = heads[head]
        q = r.xb[0, first : first + size, :, 128 * q_tile : 128 * q_tile + 128]
        return jnp.where(low if q_low else ~low, q.reshape(size * 128, 128), jnp.zeros((), BF))

    r.vt[0] = tile_of(4).T
    r.vt[1] = tile_of(1).T
    for half in range(2):
        at = slice(256 * half, 256 * half + 256)
        for head in range(3):
            scores = dot_nt(tile_of(heads[head][1]), queries(head, 2 * half, 2))
            weights = jnp.exp(scores - jnp.max(scores, axis=0, keepdims=True))
            weights = weights * (1.0 / jnp.sum(weights, axis=0, keepdims=True))
            weights = weights.astype(BF)
            r.pt[head, :, at] = weights
            out = dot(r.vt[head // 2], weights)
            if head == 0:
                r.ot[0, 0:64, at] = out[0:64]
            elif head == 1:
                r.ot[0, 64:128, at] = out[64:128]
            else:
                r.ot[1, 0:64, at] = out[64:128]
                r.ot[1, 64:128, at] = jnp.zeros((64, 256), F32)
        for k in (2 * half, 2 * half + 1):
            across = slice(128 * k, 128 * k + 128)
            r.os[k, 0:128, :] = r.ot[0, :, across].T.astype(BF)
            third = r.ot[1, 0:64, across]
            third = jnp.concatenate([third, pltpu.roll(third, 64, 1)], axis=0)
            r.os[k, 128:192, :] = third.T[0:64].astype(BF)
        for to in (2 * half, 2 * half + 1):

            @pl.when(z == to)
            def _():
                keep(r.os.at[to], r.ob.at[z], S.o)

            @pl.when(z != to)
            def _():
                push(r.os.at[to], r.ob.at[z], S.o, b, 2 * to + c)

        if half == 0:
            line_relay(out_block, S.w_out)

    sent(S.o, r.os.at[0:3])
    got(S.plane_in, r.w_in.at[:, 0, :, 0:HALF])
    line_gather(in_block, S.w_in)
    sent(S.w_in, r.w_in.at[0:3, :, :, 0:HALF])
    for k in range(2):
        r.kt[k] = tile_of(2 + k).T
    share(r.w_attn, S.group_attn, S.fw_attn)
    got(S.fw_attn, r.w_attn.at[:, 0:HALF])
    got(S.o, r.ob)
    a = jnp.zeros((ROWS, WIDTH), F32)
    for p in range(4):
        third = r.ob[p, 128:192, :].astype(F32)
        third = jnp.concatenate([third, pltpu.roll(third, 64, 1)], axis=0)
        r.o2[p] = jnp.where(low, third, 0.0).astype(BF)
        a += dot(r.ob[p, 0:128, :], r.w_attn[192 * p : 192 * p + 128, :])
        a += dot(r.o2[p, :, 0:64], r.w_attn[192 * p + 128 : 192 * p + 192, :])
    r.a[...] = a
    x1 = r.x0[...] + mod(2) * a
    r.x1[...] = x1
    n2, inv2 = normalize(x1)
    r.n2[...] = n2
    r.inv2[...] = jnp.broadcast_to(inv2, (ROWS, 128))
    r.h2[0] = (n2 * vec(1) * (1.0 + mod(4)) + mod(3)).astype(BF)
    peers(lambda k, to: push(r.h2.at[0], r.h2.at[k], S.h2 + k, to, s))
    for k in (1, 2, 3):
        sent(S.h2 + k, r.h2.at[0])
    line_relay(in_block, S.w_in)
    line_share(out_block, S.w_out, S.fw_out)
    sent(S.fw_out, r.w_out.at[:, 0])
    got(S.fw_out, r.w_out.at[:, 0])

    def feed_back(k):
        @pl.when(k > 0)
        def _():
            got(S.dm + k, r.dm.at[0])

        r.back[k] = dot_nt(r.dm[k], r.w_out[...].reshape(WIDTH, WIDTH))

    loop(4, feed_back)
    line_share(in_block, S.w_in, S.fw_in)
    sent(S.fw_in, r.w_in.at[:, :, :, 0:HALF])
    got(S.fw_in, r.w_in.at[:, :, :, 0:HALF])

    def feed(first, count):
        at = slice(first, first + count)
        size = count * ROWS
        u = dot(r.h2[at].reshape(size, WIDTH), r.w_in[...].reshape(WIDTH, WIDTH))
        slope = 0.7978845608028654
        cube = 0.044715
        t = jnp.tanh(slope * (u + cube * u * u * u))
        r.gb[at] = (0.5 * u * (1.0 + t)).astype(BF).reshape(count, ROWS, WIDTH)
        bend = 0.5 * (1.0 + t) + 0.5 * u * (1.0 - t * t) * (slope * (1.0 + 3.0 * cube * u * u))
        du = (r.back[at].reshape(size, WIDTH) * bend).astype(BF)
        r.du[at] = du.reshape(count, ROWS, WIDTH)
        r.dhs[at] = dot_nt(du, r.w_in[...].reshape(WIDTH, WIDTH)).astype(BF).reshape(count, ROWS, WIDTH)

    feed(0, 1)
    for first, count in ((1, 2), (3, 1)):
        for k in range(first, first + count):
            got(S.h2 + k, r.h2.at[0])
        feed(first, count)
        for k in range(first, first + count):
            push(r.dhs.at[k], r.dhr.at[k], S.dh2, near[k], s)
    sent(S.dh2, r.dhs.at[0:3])
    for t in range(3):
        at = slice(256 * t, 256 * t + 256)
        mm = dot(r.gb[...].reshape(512, WIDTH), r.w_out[:, :, :, at].reshape(WIDTH, 256))
        r.mms[:, :, at] = mm.astype(BF).reshape(4, ROWS, 256)

    def gather(own, others):
        total = own[0].astype(F32)
        for k in (1, 2, 3):
            total += others[k].astype(F32)
        return total

    for k in range(2):
        rows = slice(384 * k, 384 * k + 384)
        result = dot_tn(r.gb[:, :, rows].reshape(512, 384), r.dm[...].reshape(512, 768))
        r.g_out[2 * k : 2 * k + 2] = result.astype(BF).reshape(2, 2, 96, 768)
    push(r.g_out.at[:, 1 - c], r.p_out, S.pair_out, b, mate)
    sent(S.pair_out, r.p_out)

    def outer(left, right, dst):
        for k in range(2):
            rows = slice(384 * k, 384 * k + 384)
            result = dot_tn(
                left[:, :, rows].reshape(512, 384), right[...].reshape(512, 768)
            ).astype(BF)
            dst[0, rows, :] = result[:, 0:HALF]
            dst[1, rows, :] = result[:, HALF:WIDTH]

    def to_mate(grad, dst, at):
        push(grad.at[1 - c], dst, at, b, mate)
        sent(at, dst)

    def pair_sum(grad, pair, at):
        got(at, pair)
        grad[c] = (grad[c].astype(F32) + pair[...].astype(F32)).astype(BF)

    def plane_sum(grad, dst, at):
        def rows(to):
            return grad.at[c, pl.ds(pl.multiple_of(192 * to, 16), 192)]

        peers(lambda k, to: push(rows(to), dst.at[k], at, to, s))
        keep(rows(b), dst.at[0], at)
        sent(at, dst.at[0:3])

    def line_sum(src, total, dst, first, at):
        got(first, src)
        total[...] = (
            (src[0].astype(F32) + src[1].astype(F32)) + (src[2].astype(F32) + src[3].astype(F32))
        ).astype(BF)

        def rows(to):
            return total.at[pl.ds(pl.multiple_of(48 * to, 16), 48)]

        stack(lambda to: push(rows(to), dst.at[z], at, b, 2 * to + c))
        keep(rows(z), dst.at[z], at)
        sent(at, dst.at[0:3])

    def trade(total, final, at):
        push(total.at[:, mate24], final.at[:, c], at, b, mate)
        sent(at, final.at[:, 0])
        final[:, c] = total[:, own24, :]

    for k in range(2):
        rows = slice(384 * k, 384 * k + 384)
        result = dot_tn(r.h2[:, :, rows].reshape(512, 384), r.du[...].reshape(512, 768)).astype(BF)
        for h in range(2):
            r.g_in[h, 2 * k : 2 * k + 2] = result[:, 384 * h : 384 * h + 384].reshape(2, 4, 48, 384)
    to_mate(r.g_in, r.p_in, S.pair_in)

    got(S.pair_out, r.p_out)
    for k in range(4):
        r.g_out[k, c] = (r.g_out[k, c].astype(F32) + r.p_out[k].astype(F32)).astype(BF)

    def out_rows(k):
        return r.g_out.at[k, c]

    for j in (0, 1):
        line_add(j, out_rows, r.r_out, r.via_out, S.line_out)

    def add_out():
        k = line_order(2)
        r.g_out[k, c] = (r.g_out[k, c].astype(F32) + r.via_out[...].astype(F32)).astype(BF)

    got(S.dh2, r.dhr.at[0:3])
    dh = gather(r.dhs, r.dhr)
    n2 = r.n2[...]
    inv2 = r.inv2[:, 0:1]
    r.early[...] = jnp.zeros((8, 768), F32)
    r.early[2:3, :] = jnp.sum(dh, axis=0, keepdims=True)
    both = jnp.sum(dh * n2, axis=0, keepdims=True)
    r.early[3:4, :] = both * vec(1)
    r.early[0:1, :] = both * (1.0 + mod(4))
    grad = dh * ((1.0 + mod(4)) * vec(1))
    dx1 = i_cot[0].astype(F32) + norm_back(n2, inv2, grad)
    r.dx1[...] = dx1
    r.early[1:2, :] = jnp.sum(dx1 * r.a[...], axis=0, keepdims=True)
    r.das[...] = (dx1 * mod(2)).astype(BF)
    for p in range(4):
        first = 192 * p
        r.dos[p, 0:128, :] = dot_nt(r.das[...], r.w_attn[first : first + 128, :]).astype(BF)
        tail = dot_nt(r.das[...], r.w_attn[first + 128 : first + 192, :])
        tail = jnp.concatenate([tail, jnp.zeros((ROWS, 64), F32)], axis=1)
        r.dos[p, 128:192, :] = jnp.where(low, tail[0:64], pltpu.roll(tail[64:128], 64, 1)).astype(
            BF
        )

    stack(lambda to: push(r.dos.at[to], r.dob.at[z], S.do, b, 2 * to + c))
    keep(r.dos.at[z], r.dob.at[z], S.do)
    sent(S.do, r.dos.at[0:3])
    peers(lambda k, to: push(r.mms.at[k], r.mmr.at[k], S.mm, to, s))
    sent(S.mm, r.mms.at[0:3])

    for p in range(4):
        for rows, left_side in (
            (slice(192 * p, 192 * p + 128), r.ob[p, 0:128, :]),
            (slice(192 * p + 128, 192 * p + 192), r.o2[p]),
        ):
            result = dot_tn(left_side, r.das[...])[0 : rows.stop - rows.start].astype(BF)
            r.g_attn[0, rows, :] = result[:, 0:HALF]
            r.g_attn[1, rows, :] = result[:, HALF:WIDTH]
    to_mate(r.g_attn, r.p_attn, S.pair_attn)

    def over_line(src, dst, name):
        def one(k):
            push(src, dst.at[s], name, b, lax.rem(s + k, SEQ))

        loop(SEQ, one, 1)
        keep(src, dst.at[s], name)
        sent(name, dst.at[0:7])

    def over_group(got_ref, dst, name):
        total = got_ref[0]
        for k in range(1, SEQ):
            total += got_ref[k]
        dst[b] = total
        peers(lambda k, to: push(dst.at[b], dst.at[b], name, to, s))
        sent(name, dst.at[0:3])


    pair_sum(r.g_in, r.p_in, S.pair_in)

    line_via(r.via_out, S.line_out, add_out)
    for j in (2, 3):
        line_add(j, out_rows, r.r_out, r.via_out, S.line_out)
    sent(S.line_out, r.r_out.at[0:3])

    def in_rows(k):
        return r.g_in.at[c, :, k]

    for j in (0, 1):
        line_add(j, in_rows, r.r_in, r.via_in, S.line_in)

    def add_in():
        k = line_order(2)
        r.g_in[c, :, k] = (r.g_in[c, :, k].astype(F32) + r.via_in[...].astype(F32)).astype(BF)

    pair_sum(r.g_attn, r.p_attn, S.pair_attn)
    plane_sum(r.g_attn, r.q_attn, S.plane_attn)

    got(S.do, r.dob)
    dot0 = r.dob[:, 0:128, :].reshape(512, 128)
    third = r.dob[:, 128:192, :].astype(F32).reshape(256, 128)
    other_rows = jnp.where(low, pltpu.roll(third, 64, 1), 0.0).reshape(4, 64, 128)
    third = jnp.where(low, third, 0.0).reshape(4, 64, 128)
    dot1 = jnp.concatenate([third, other_rows], axis=1).reshape(512, 128)
    zero = jnp.zeros((), BF)
    moved = pltpu.roll(dot1, 64, 1).astype(BF)
    grads = (jnp.where(low, dot0, zero), jnp.where(low, zero, dot0), moved)
    product = dot0.astype(F32).T * r.ot[0]
    deltas = (
        jnp.sum(product[0:64], axis=0, keepdims=True),
        jnp.sum(product[64:128], axis=0, keepdims=True),
        jnp.sum(dot1.T * r.ot[1], axis=0, keepdims=True),
    )
    for head in range(3):
        values = tile_of(heads[head][2])
        for half in range(2):
            at = slice(256 * half, 256 * half + 256)
            dp = dot_nt(values, grads[head][at])
            r.dst[head, :, at] = (
                r.pt[head, :, at].astype(F32) * (dp - deltas[head][:, at])
            ).astype(BF)

    def key_grads(rows):
        dk = [dot(r.dst[head, rows, :], queries(head, 0, 4)) for head in range(3)]
        dv = [dot(r.pt[head, rows, :], grads[head]) for head in range(3)]
        return (dv[2], dk[0] + dk[1], dk[2], dv[0] + dv[1])

    line_via(r.via_in, S.line_in, add_in)
    for j in (2, 3):
        line_add(j, in_rows, r.r_in, r.via_in, S.line_in)
    sent(S.line_in, r.r_in.at[0:3])
    for t, tile in enumerate(key_grads(slice(512, 1024))):
        r.gps[:, 128 * t : 128 * t + 128] = tile.astype(BF)
    push(r.gps, r.gpr, S.gp, b, mate)
    sent(S.gp, r.gps)
    for t, tile in enumerate(key_grads(slice(0, 512))):
        r.ga[:, 128 * t + 128 : 128 * t + 256] = tile
    for half in range(2):
        at = slice(256 * half, 256 * half + 256)
        turned_q = [dot(r.kt[head // 2], r.dst[head, :, at]) for head in range(3)]
        top = jnp.concatenate([turned_q[0][0:64], turned_q[1][64:128]], axis=0)
        r.ga[at, 0:128] = top.T * 0.125
        r.ga[at, 128:256] += turned_q[2].T * 0.125
    got(S.mm, r.mmr.at[0:3])
    mm = gather(r.mms, r.mmr)
    o_y[...] = (r.x1[...] + mod(5) * mm).astype(BF)
    r.early[4:5, :] = jnp.sum(i_cot[0].astype(F32) * mm, axis=0, keepdims=True)
    over_line(r.early, r.early_got, S.early)
    got(S.gp, r.gpr)

    def dh1_rows(k):
        return r.d1s.at[k]

    def back_turn(k):
        rows = pl.ds(pl.multiple_of(128 * k, 128), 128)
        tiles = [r.ga[rows, 0:128]] + [
            r.ga[rows, 128 * t : 128 * t + 128]
            + r.gpr[rows, 128 * t - 128 : 128 * t].astype(F32)
            for t in range(1, 5)
        ]
        tiles[0] = turned(tiles[0], -1.0, k)
        tiles[1] = jnp.where(low, turned(tiles[1], -1.0, k), tiles[1])
        tiles[2] = turned(tiles[2], -1.0, k)
        tiles[3] = turned(tiles[3], -1.0, k)
        for t in range(5):
            r.dqkv[k, :, 128 * t : 128 * t + 128] = tiles[t].astype(BF)
        r.dqkv[k, :, PACK:WIDTH] = jnp.zeros((128, 128), BF)

    loop(4, back_turn)

    def unproject(j):
        k = line_order(j)
        partial_sum = dot_nt(r.dqkv[k, :, 0:PACK], r.w_qkv[:, 0:PACK])
        r.d1s[k] = partial_sum.astype(BF)
        if j == 2:

            def add():
                r.d1s[k] = (partial_sum + r.via_dh1[...].astype(F32)).astype(BF)

            line_via(r.via_dh1, S.dh1, add)
        line_add(j, dh1_rows, r.d1r, r.via_dh1, S.dh1)

    unproject(0)
    outer(r.h1, r.dqkv, r.g_qkv)
    to_mate(r.g_qkv, r.p_qkv, S.pair_qkv)
    unproject(1)
    pair_sum(r.g_qkv, r.p_qkv, S.pair_qkv)
    plane_sum(r.g_qkv, r.q_qkv, S.plane_qkv)
    unproject(2)
    unproject(3)
    sent(S.dh1, r.d1s.at[0:3])
    line_sum(r.q_attn, r.m_attn, r.r_attn, S.plane_attn, S.line_attn)
    got(S.early, r.early_got)
    over_group(r.early_got, r.early_all, S.early2)

    line_done(r.r_in, S.line_in)
    r.m_in[...] = (
        (r.r_in[0].astype(F32) + r.r_in[1].astype(F32))
        + (r.r_in[2].astype(F32) + r.r_in[3].astype(F32))
    ).astype(BF)
    peers(lambda k, to: push(r.m_in.at[to], r.u_in.at[b], S.slice_in, to, s))
    keep(r.m_in.at[b], r.u_in.at[b], S.slice_in)
    sent(S.slice_in, r.u_in.at[0:3])
    line_sum(r.q_qkv, r.m_qkv, r.r_qkv, S.plane_qkv, S.line_qkv)

    line_done(r.d1r, S.dh1)
    dh = (r.d1r[0].astype(F32) + r.d1r[1].astype(F32)) + (
        r.d1r[2].astype(F32) + r.d1r[3].astype(F32)
    )
    n1 = r.n1[...]
    both = jnp.sum(dh * n1, axis=0, keepdims=True)
    r.late[0:1, :] = both * (1.0 + mod(1))
    r.late[1:2, :] = jnp.sum(dh, axis=0, keepdims=True)
    r.late[2:3, :] = both * vec(0)
    grad = dh * ((1.0 + mod(1)) * vec(0))
    dx0 = r.dx1[...] + norm_back(n1, r.inv1[:, 0:1], grad)
    _, hidden = start_tokens(i_tok[0], z)
    o_dx[...] = jnp.where(hidden, 0.0, dx0)
    r.late[3:4, :] = jnp.sum(jnp.where(hidden, dx0, 0.0), axis=0, keepdims=True)
    over_line(r.late, r.late_got, S.late)

    line_done(r.r_out, S.line_out)
    total = (r.r_out[0].astype(F32) + r.r_out[1].astype(F32)) + (
        r.r_out[2].astype(F32) + r.r_out[3].astype(F32)
    )
    o_gout[...] = total
    squares = total * total
    squares = jnp.sum(squares[:, 0:128] + squares[:, 128:256] + squares[:, 256:384]
                      + squares[:, 384:512] + squares[:, 512:640] + squares[:, 640:768],
                      axis=0, keepdims=True)

    def fold(value):
        total = value[:, 0:128] * value[:, 0:128]
        for t in range(1, value.shape[1] // 128):
            total += value[:, 128 * t : 128 * t + 128] * value[:, 128 * t : 128 * t + 128]
        return jnp.sum(total, axis=0, keepdims=True)

    got(S.slice_in, r.u_in)
    r.t_in[...] = r.u_in[...].astype(F32)
    trade(r.t_in, r.f_in, S.last_in)
    got(S.line_attn, r.r_attn)
    r.t_attn[0] = (r.r_attn[0].astype(F32) + r.r_attn[1].astype(F32)) + (
        r.r_attn[2].astype(F32) + r.r_attn[3].astype(F32)
    )
    trade(r.t_attn, r.f_attn, S.last_attn)
    got(S.line_qkv, r.r_qkv)
    r.t_qkv[...] = r.r_qkv[...].astype(F32)
    trade(r.t_qkv, r.f_qkv, S.last_qkv)
    got(S.late, r.late_got)
    over_group(r.late_got, r.late_all, S.late2)
    got(S.last_in, r.f_in.at[:, 0])
    got(S.last_attn, r.f_attn.at[:, 0])
    for h in range(2):
        for p in range(4):
            value = r.f_in[p, h]
            o_gin[:, 768 * p + 384 * h : 768 * p + 384 * h + 384] = value
            squares += fold(value)
        value = r.f_attn[0, h]
        o_gattn[:, 384 * h : 384 * h + 384] = value
        squares += fold(value)
    got(S.last_qkv, r.f_qkv.at[:, 0])
    where = {which: index for index, which in enumerate(HALVES) if which is not None}

    def packed_half(chunk, high):
        kind, rest = chunk // 12, chunk % 12
        index = where[(kind, rest % 3)]
        t = index // 2
        tile = r.f_qkv[rest // 3, t // 3, :, t % 3 * 128 : t % 3 * 128 + 128]
        return tile if index % 2 == high else pltpu.roll(tile, 64, 1)

    for t in range(18):
        o_gqkv[:, 128 * t : 128 * t + 128] = jnp.where(
            low, packed_half(2 * t, 0), packed_half(2 * t + 1, 1)
        )
    for p in range(4):
        for h in range(2):
            squares += fold(r.f_qkv[p, h])

    r.sq[me] = squares

    def send_sq(k):
        other = lax.rem(me + k, ALL)
        push(r.sq.at[me], r.sq.at[me], S.sq, lax.div(other, SEQ), lax.rem(other, SEQ))

    loop(ALL, send_sq, 1)
    sent(S.sq, r.sq.at[0:31])
    got(S.early2, r.early_all.at[0:3])
    got(S.late2, r.late_all.at[0:3])
    mods = []
    for k in range(4):
        early, late = r.early_all[k], r.late_all[k]
        rows = jnp.concatenate([late[1:3], early[1:5], jnp.zeros((2, 768), F32)], axis=0)
        for n in range(6):
            for m in range(6):
                r.dmod_flat[k, 6 * n + m : 6 * n + m + 1, :] = rows[
                    n : n + 1, 128 * m : 128 * m + 128
                ]
        mods.append(rows)
    gain = jnp.concatenate(
        [
            sum(r.late_all[k][0:1] for k in range(4)),
            sum(r.early_all[k][0:1] for k in range(4)),
            (mods[0] + mods[1] + mods[2] + mods[3])[0:6],
        ],
        axis=0,
    )
    mask_row = sum(r.late_all[k][3:4] for k in range(4))
    gains = jnp.concatenate([gain, mask_row, jnp.zeros((7, 768), F32)], axis=0)
    masters = jnp.concatenate([i_vec[...], jnp.zeros((7, 768), F32)], axis=0)
    own = lax.rem(WIDTH - 24 * me, WIDTH)
    o_gvec[...] = pltpu.roll(gains, own, 1)[:, 0:128]
    o_vec[...] = pltpu.roll(masters, own, 1)[:, 0:128]
    r.mod_pad[...] = jnp.zeros((8, 384), F32)
    window = lax.div(wide * me, 128)
    for k in range(4):
        rows = r.dmod_flat[k, pl.ds(window, 3), :]
        for m in range(3):
            r.mod_pad[k : k + 1, 128 * m : 128 * m + 128] = rows[m : m + 1, :]
    o_dmod[...] = pltpu.roll(r.mod_pad[...], lax.rem(384 - lax.rem(wide * me, 128), 384), 1)[:, 0:256]
    small = jnp.sum(gain * gain) + jnp.sum(mask_row * mask_row)
    conds = [r.conds_all[k][0:1].astype(BF).astype(F32) for k in range(4)]
    for k in range(4):
        for m in range(k, 4):
            term = jnp.sum(mods[k] * mods[m]) * jnp.sum(conds[k] * conds[m])
            small += term if m == k else 2.0 * term
    got(S.sq, r.sq.at[0:31])
    total = r.sq[0]
    for k in range(1, ALL):
        total += r.sq[k]
    o_norm[...] = jnp.broadcast_to(jnp.sqrt(jnp.sum(total) + small), (8, 128))

    for at, like in drains:
        left(at, like)


def run_layer(*args):
    shapes = (
        ((ROWS, WIDTH), BF),
        ((ROWS, WIDTH), F32),
        ((8, 128), F32),
        ((24, 3 * WIDTH), F32),
        ((24, WIDTH), F32),
        ((24, 4 * WIDTH), F32),
        ((96, WIDTH), F32),
        ((8, 256), F32),
        ((16, 128), F32),
        ((16, 128), F32),
        ((8, 128), F32),
    )
    whole = pl.BlockSpec(memory_space=pltpu.VMEM)
    return pl.pallas_call(
        layer_kernel,
        out_shape=[jax.ShapeDtypeStruct(shape, kind) for shape, kind in shapes],
        in_specs=[pl.BlockSpec(memory_space=pl.ANY)] * 3 + [whole] * (len(args) - 3),
        out_specs=[whole] * len(shapes),
        scratch_shapes=[pltpu.VMEM(shape, kind) for shape, kind in SCRATCH.values()]
        + [pltpu.SMEM((3, 1), jnp.int32)]
        + [pltpu.SemaphoreType.DMA((SEM_COUNT,)), pltpu.SemaphoreType.DMA((SEM_COUNT,))],
        compiler_params=pltpu.CompilerParams(
            collective_id=0, has_side_effects=True, vmem_limit_bytes=60 * 1024 * 1024
        ),
    )(*args)


def finish_kernel(
    y, dx, norm, g_qkv, g_attn, g_in, g_out, dmod, g_vec, own_vec, conds, *rest
):
    (w_ada, w_qkv, w_attn, w_in, w_out), moments, outs = rest[:5], rest[5:17], rest[17:]
    outs[0][0] = y[...]
    outs[1][0] = dx[...]
    outs[2][0, 0] = norm[0, 0]
    clip = jnp.minimum(1.0, CLIP / (norm[0:1, 0:1] + 1e-06))
    columns = w_ada.shape[0]
    rounded = conds[...].astype(BF).astype(F32)
    turned_mod = dmod[...].T
    g_ada = turned_mod[0:columns, 0:1] * rounded[0:1, :]
    for k in range(1, 4):
        g_ada += turned_mod[0:columns, k : k + 1] * rounded[k : k + 1, :]
    narrow = moments[0].shape[1]
    grads = (
        g_vec[0:9, 0:narrow],
        g_ada,
        g_qkv[...],
        g_attn[...],
        g_in[...],
        g_out[...],
    )
    weights = (
        own_vec[0:9, 0:narrow],
        w_ada[...],
        w_qkv[...],
        w_attn[...],
        w_in[...],
        w_out[...],
    )
    for k in range(6):
        results = adam_step(
            weights[k],
            grads[k] * clip,
            moments[2 * k][...],
            moments[2 * k + 1][...],
            RATE if k else RATE_VECTORS,
            DECAY if k else 0.0,
        )
        for n in range(3):
            outs[3 + 3 * k + n][...] = results[n]


def run_finish(partial_results, weights, moments):
    shapes = [((1, ROWS, WIDTH), BF), ((1, ROWS, WIDTH), F32), ((1, 1), F32)]
    for moment in moments[::2]:
        shapes += [(moment.shape, F32)] * 3
    whole = pl.BlockSpec(memory_space=pltpu.VMEM)
    specs = [whole] * len(shapes)
    specs[2] = pl.BlockSpec(memory_space=pltpu.SMEM)
    args = (*partial_results, *weights, *moments)
    return pl.pallas_call(
        finish_kernel,
        out_shape=[jax.ShapeDtypeStruct(shape, kind) for shape, kind in shapes],
        in_specs=[whole] * len(args),
        out_specs=specs,
        compiler_params=pltpu.CompilerParams(vmem_limit_bytes=60 * 1024 * 1024),
    )(*args)


def slices(
    tokens_in,
    cotangent,
    timesteps,
    span_start,
    span_len,
    vectors,
    w_ada,
    w_qkv,
    w_attn,
    w_in,
    w_out,
    m_vec,
    v_vec,
    m_ada,
    v_ada,
    m_qkv,
    v_qkv,
    m_attn,
    v_attn,
    m_in,
    v_in,
    m_out,
    v_out,
):
    partial_results = run_layer(
        timesteps,
        span_start,
        span_len,
        tokens_in,
        cotangent,
        vectors,
        w_ada.T,
        w_qkv,
        w_attn,
        w_in,
        w_out,
    )
    moments = (
        m_vec,
        v_vec,
        m_ada.T,
        v_ada.T,
        m_qkv,
        v_qkv,
        m_attn,
        v_attn,
        m_in,
        v_in,
        m_out,
        v_out,
    )
    results = run_finish(partial_results, (w_ada.T, w_qkv, w_attn, w_in, w_out), moments)
    ada_results = [result.T for result in results[6:9]]
    return (*results[:2], results[2].reshape(()), *results[3:6], *ada_results, *results[9:])


def solution(mesh):
    in_specs = (
        P("dp", "seq", None),
        P("dp", "seq", None),
        P("dp"),
        P("dp"),
        P("dp"),
        P(),
        P(None, ("dp", "seq")),
        P(("dp", "seq"), None),
        P(("dp", "seq"), None),
        P(("dp", "seq"), None),
        P(("dp", "seq"), None),
        P(None, ("dp", "seq")),
        P(None, ("dp", "seq")),
        P(None, ("dp", "seq")),
        P(None, ("dp", "seq")),
        P(("dp", "seq"), None),
        P(("dp", "seq"), None),
        P(("dp", "seq"), None),
        P(("dp", "seq"), None),
        P(("dp", "seq"), None),
        P(("dp", "seq"), None),
        P(("dp", "seq"), None),
        P(("dp", "seq"), None),
    )
    out_specs = (
        P("dp", "seq", None),
        P("dp", "seq", None),
        P(),
        P(None, ("dp", "seq")),
        P(None, ("dp", "seq")),
        P(None, ("dp", "seq")),
        P(None, ("dp", "seq")),
        P(None, ("dp", "seq")),
        P(None, ("dp", "seq")),
        P(("dp", "seq"), None),
        P(("dp", "seq"), None),
        P(("dp", "seq"), None),
        P(("dp", "seq"), None),
        P(("dp", "seq"), None),
        P(("dp", "seq"), None),
        P(("dp", "seq"), None),
        P(("dp", "seq"), None),
        P(("dp", "seq"), None),
        P(("dp", "seq"), None),
        P(("dp", "seq"), None),
        P(("dp", "seq"), None),
    )
    sizes = dict(mesh.shape)
    local = slices if (sizes["dp"], sizes["seq"]) == (4, 8) else plain
    return jax.shard_map(local, mesh=mesh, in_specs=in_specs, out_specs=out_specs, check_vma=False)
```

```python
from functools import partial
import math
from types import SimpleNamespace

import jax
import jax.numpy as jnp
from jax import lax
from jax.experimental import pallas as pl
from jax.experimental.pallas import tpu as pltpu
from jax.sharding import PartitionSpec as P

HD = 64
COND = 128
STEP = 10


BETA_ONE = 0.9
BETA_TWO = 0.999
ADAM_EPS = 1e-08
RATE = 0.1
RATE_VECTORS = 0.3
DECAY = 0.01
CLIP = 1.0
NORM_EPS = 1e-05


def cond_input(timesteps):
    half_cond = COND // 2
    freqs = jnp.exp(jnp.arange(half_cond, dtype=jnp.float32) * (-math.log(10000.0) / half_cond))
    angles = timesteps.astype(jnp.float32)[:, None] * freqs[None, :]
    return jax.nn.silu(jnp.concatenate([jnp.cos(angles), jnp.sin(angles)], axis=1))


def rotary_tables(positions):
    half_head = HD // 2
    inverse = jnp.exp(jnp.arange(half_head, dtype=jnp.float32) * (-math.log(10000.0) / half_head))
    angles = positions.astype(jnp.float32)[:, None] * inverse[None, :]
    return (jnp.cos(angles), jnp.sin(angles))


def rotate(values, cosines, sines):
    half_head = values.shape[-1] // 2
    first = values[..., :half_head]
    second = values[..., half_head:]
    cos_b = cosines[:, None, :]
    sin_b = sines[:, None, :]
    return jnp.concatenate(
        [first * cos_b - second * sin_b, second * cos_b + first * sin_b], axis=-1
    )


def rotate_back(grads, cosines, sines):
    half_head = grads.shape[-1] // 2
    first = grads[..., :half_head]
    second = grads[..., half_head:]
    cos_b = cosines[:, None, :]
    sin_b = sines[:, None, :]
    return jnp.concatenate(
        [first * cos_b + second * sin_b, second * cos_b - first * sin_b], axis=-1
    )


def normalize(values):
    centre = jnp.mean(values, axis=-1, keepdims=True)
    centred = values - centre
    inverse = lax.rsqrt(jnp.mean(centred * centred, axis=-1, keepdims=True) + NORM_EPS)
    return (centred * inverse, inverse)


def norm_back(normed, inverse, grad):
    return inverse * (
        grad
        - jnp.mean(grad, axis=-1, keepdims=True)
        - normed * jnp.mean(grad * normed, axis=-1, keepdims=True)
    )


def split_kv(block, width):
    seqs, block_rows = (block.shape[0], block.shape[1])
    keys = block[..., :width].reshape(seqs, block_rows, width // HD, HD)
    values = block[..., width:].reshape(seqs, block_rows, width // HD, HD)
    return (keys, values)


def attend_piece(carry, piece, queries, width, factor):
    piece_rows = piece.shape[1]
    size = math.gcd(piece_rows, 512)

    def attend_one_block(index, state):
        running, denom, accum = state
        block = lax.dynamic_slice_in_dim(piece, index * size, size, 1)
        keys, values = split_kv(block, width)
        scores = (
            jnp.einsum("sqhd,skhd->shqk", queries, keys, preferred_element_type=jnp.float32)
            * factor
        )
        highest = jnp.maximum(running, jnp.max(scores, axis=-1))
        shrink = jnp.exp(running - highest)
        weights = jnp.exp(scores - highest[..., None])
        denom = denom * shrink + jnp.sum(weights, axis=-1)
        accum = accum * shrink[..., None] + jnp.einsum(
            "shqk,skhd->shqd",
            weights.astype(jnp.bfloat16),
            values,
            preferred_element_type=jnp.float32,
        )
        return (highest, denom, accum)

    return lax.fori_loop(0, piece_rows // size, attend_one_block, carry)


def block_grads(block, queries, grad_out, logsum, delta, width, factor):
    keys, values = split_kv(block, width)
    scores = (
        jnp.einsum("sqhd,skhd->shqk", queries, keys, preferred_element_type=jnp.float32) * factor
    )
    probs = jnp.exp(scores - logsum[..., None])
    dprobs = jnp.einsum("sqhd,skhd->shqk", grad_out, values, preferred_element_type=jnp.float32)
    dscores = (probs * (dprobs - delta[..., None])).astype(jnp.bfloat16)
    return (keys, probs, dscores)


def query_grads(kv_all, queries, grad_out, logsum, delta, width, factor):
    total_rows = kv_all.shape[1]
    size = math.gcd(total_rows, 512)

    def query_one_block(index, accum):
        block = lax.dynamic_slice_in_dim(kv_all, index * size, size, 1)
        keys, probs, dscores = block_grads(block, queries, grad_out, logsum, delta, width, factor)
        return accum + factor * jnp.einsum(
            "shqk,skhd->sqhd", dscores, keys, preferred_element_type=jnp.float32
        )

    return lax.fori_loop(
        0, total_rows // size, query_one_block, jnp.zeros(queries.shape, jnp.float32)
    )


def key_grads(kv_all, queries, grad_out, logsum, delta, width, factor, count):
    size = math.gcd(count, 512)
    seqs = queries.shape[0]

    def key_one_block(index, accum):
        block = lax.dynamic_slice_in_dim(kv_all, index * size, size, 1)
        keys, probs, dscores = block_grads(block, queries, grad_out, logsum, delta, width, factor)
        grad_vals = jnp.einsum(
            "shqk,sqhd->skhd",
            probs.astype(jnp.bfloat16),
            grad_out,
            preferred_element_type=jnp.float32,
        )
        grad_keys = factor * jnp.einsum(
            "shqk,sqhd->skhd", dscores, queries, preferred_element_type=jnp.float32
        )
        joined = jnp.concatenate(
            [grad_keys.reshape(seqs, size, width), grad_vals.reshape(seqs, size, width)], axis=-1
        )
        return lax.dynamic_update_slice_in_dim(
            accum, jnp.transpose(joined, (1, 0, 2)), index * size, 0
        )

    initial = jnp.zeros((count, seqs, 2 * width), jnp.float32)
    return lax.fori_loop(0, count // size, key_one_block, initial)


def adam_step(weight, grad, first, second, rate, decay_rate):
    new_first = BETA_ONE * first + (1.0 - BETA_ONE) * grad
    new_second = BETA_TWO * second + (1.0 - BETA_TWO) * grad * grad
    fixed_first = new_first / (1.0 - BETA_ONE**STEP)
    fixed_second = new_second / (1.0 - BETA_TWO**STEP)
    new_weight = weight - rate * (
        fixed_first / (jnp.sqrt(fixed_second) + ADAM_EPS) + decay_rate * weight
    )
    return (new_first, new_second, new_weight)


def mod_back(grad_hidden, ln_values, normed, scale_part, gain):
    grad_shift = jnp.sum(grad_hidden, axis=1)
    grad_scale = jnp.sum(grad_hidden * ln_values, axis=1)
    grad_ln = grad_hidden * (1.0 + scale_part)
    grad_gain = jnp.sum(grad_ln * normed, axis=(0, 1))
    return (grad_shift, grad_scale, grad_gain, grad_ln * gain)


def plain(
    tokens_in,
    cotangent,
    timesteps,
    span_start,
    span_len,
    vectors,
    w_ada,
    w_qkv,
    w_attn,
    w_in,
    w_out,
    m_vec,
    v_vec,
    m_ada,
    v_ada,
    m_qkv,
    v_qkv,
    m_attn,
    v_attn,
    m_in,
    v_in,
    m_out,
    v_out,
):
    seqs, group, width = tokens_in.shape
    heads = width // HD
    factor = HD ** (-0.5)
    flat_rows = seqs * group
    full_ada, full_qkv, full_attn, full_in, full_out = (
        lax.all_gather(w_ada.astype(jnp.bfloat16), ("dp", "seq"), axis=1, tiled=True),
        lax.all_gather(w_qkv.astype(jnp.bfloat16), ("dp", "seq"), axis=0, tiled=True),
        lax.all_gather(w_attn.astype(jnp.bfloat16), ("dp", "seq"), axis=0, tiled=True),
        lax.all_gather(w_in.astype(jnp.bfloat16), ("dp", "seq"), axis=0, tiled=True),
        lax.all_gather(w_out.astype(jnp.bfloat16), ("dp", "seq"), axis=0, tiled=True),
    )
    positions = lax.axis_index("seq") * group + jnp.arange(group, dtype=jnp.int32)
    masked = (positions[None, :] >= span_start[:, None]) & (
        positions[None, :] < (span_start + span_len)[:, None]
    )
    cond_bf = cond_input(timesteps).astype(jnp.bfloat16)
    modulation = jnp.dot(cond_bf, full_ada, preferred_element_type=jnp.float32) + vectors[
        2:8
    ].reshape(1, 6 * width)
    pieces = [modulation[:, which * width : (which + 1) * width][:, None, :] for which in range(6)]
    shift_one, scale_one, gate_one, shift_two, scale_two, gate_two = pieces
    start_tokens = jnp.where(
        masked[..., None], vectors[8][None, None, :], tokens_in.astype(jnp.float32)
    )
    normed_one, inv_one = normalize(start_tokens)
    ln_one = normed_one * vectors[0]
    hidden_one = (
        (ln_one * (1.0 + scale_one) + shift_one).astype(jnp.bfloat16).reshape(flat_rows, width)
    )
    projected = jnp.dot(hidden_one, full_qkv, preferred_element_type=jnp.float32).reshape(
        seqs, group, 3 * width
    )
    cosines, sines = rotary_tables(positions)
    queries = rotate(projected[..., :width].reshape(seqs, group, heads, HD), cosines, sines).astype(
        jnp.bfloat16
    )
    keys_here = rotate(
        projected[..., width : 2 * width].reshape(seqs, group, heads, HD), cosines, sines
    ).astype(jnp.bfloat16)
    values_here = projected[..., 2 * width :].astype(jnp.bfloat16)
    kv_local = jnp.concatenate([keys_here.reshape(seqs, group, width), values_here], axis=-1)
    initial = (
        jnp.full((seqs, heads, group), -1e30, jnp.float32),
        jnp.zeros((seqs, heads, group), jnp.float32),
        jnp.zeros((seqs, heads, group, HD), jnp.float32),
    )
    running, denom, accum = attend_piece(
        initial, lax.all_gather(kv_local, "seq", axis=1, tiled=True), queries, width, factor
    )
    attn_heads = accum / denom[..., None]
    logsum = running + jnp.log(denom)
    attn_rows = jnp.transpose(attn_heads, (0, 2, 1, 3)).reshape(flat_rows, width)
    attn_bf = attn_rows.astype(jnp.bfloat16)
    branch_one = jnp.dot(attn_bf, full_attn, preferred_element_type=jnp.float32).reshape(
        seqs, group, width
    )
    mid_tokens = start_tokens + gate_one * branch_one
    normed_two, inv_two = normalize(mid_tokens)
    ln_two = normed_two * vectors[1]
    hidden_two = (
        (ln_two * (1.0 + scale_two) + shift_two).astype(jnp.bfloat16).reshape(flat_rows, width)
    )
    pre_act = jnp.dot(hidden_two, full_in, preferred_element_type=jnp.float32)
    activ, gelu_back = jax.vjp(partial(jax.nn.gelu, approximate=True), pre_act)
    activ_bf = activ.astype(jnp.bfloat16)
    branch_two = jnp.dot(activ_bf, full_out, preferred_element_type=jnp.float32).reshape(
        seqs, group, width
    )
    block_out = (mid_tokens + gate_two * branch_two).astype(jnp.bfloat16)
    grad_y = cotangent.astype(jnp.float32)
    grad_gate_two = jnp.sum(grad_y * branch_two, axis=1)
    grad_branch_two = (grad_y * gate_two).astype(jnp.bfloat16).reshape(flat_rows, width)
    grad_w_out = jnp.dot(activ_bf.T, grad_branch_two, preferred_element_type=jnp.float32)
    grad_activ = jnp.dot(grad_branch_two, full_out.T, preferred_element_type=jnp.float32)
    grad_pre = gelu_back(grad_activ)[0].astype(jnp.bfloat16)
    grad_w_in = jnp.dot(hidden_two.T, grad_pre, preferred_element_type=jnp.float32)
    grad_hidden_two = jnp.dot(grad_pre, full_in.T, preferred_element_type=jnp.float32).reshape(
        seqs, group, width
    )
    grad_shift_two, grad_scale_two, grad_gain_two, grad_normed_two = mod_back(
        grad_hidden_two, ln_two, normed_two, scale_two, vectors[1]
    )
    grad_mid = grad_y + norm_back(normed_two, inv_two, grad_normed_two)
    grad_gate_one = jnp.sum(grad_mid * branch_one, axis=1)
    grad_branch_one = (grad_mid * gate_one).astype(jnp.bfloat16).reshape(flat_rows, width)
    grad_w_attn = jnp.dot(attn_bf.T, grad_branch_one, preferred_element_type=jnp.float32)
    grad_attn_bf = (
        jnp.dot(grad_branch_one, full_attn.T, preferred_element_type=jnp.float32)
        .astype(jnp.bfloat16)
        .reshape(seqs, group, heads, HD)
    )
    delta = jnp.einsum("sqhd,shqd->shq", grad_attn_bf.astype(jnp.float32), attn_heads)
    kv_all = lax.all_gather(kv_local, "seq", axis=1, tiled=True)
    grad_queries = query_grads(kv_all, queries, grad_attn_bf, logsum, delta, width, factor)
    grad_kv = jnp.transpose(
        lax.psum_scatter(
            key_grads(
                kv_all,
                queries,
                grad_attn_bf,
                logsum,
                delta,
                width,
                factor,
                group * lax.axis_size("seq"),
            ).astype(jnp.bfloat16),
            "seq",
            scatter_dimension=0,
            tiled=True,
        ).astype(jnp.float32),
        (1, 0, 2),
    )
    grad_keys = grad_kv[..., :width].reshape(seqs, group, heads, HD)
    grad_qkv = jnp.concatenate(
        [
            rotate_back(grad_queries, cosines, sines).reshape(seqs, group, width),
            rotate_back(grad_keys, cosines, sines).reshape(seqs, group, width),
            grad_kv[..., width:],
        ],
        axis=-1,
    )
    grad_qkv = grad_qkv.astype(jnp.bfloat16).reshape(flat_rows, 3 * width)
    grad_w_qkv = jnp.dot(hidden_one.T, grad_qkv, preferred_element_type=jnp.float32)
    grad_hidden_one = jnp.dot(grad_qkv, full_qkv.T, preferred_element_type=jnp.float32).reshape(
        seqs, group, width
    )
    grad_shift_one, grad_scale_one, grad_gain_one, grad_normed_one = mod_back(
        grad_hidden_one, ln_one, normed_one, scale_one, vectors[0]
    )
    grad_start = grad_mid + norm_back(normed_one, inv_one, grad_normed_one)
    grad_mask_row = jnp.sum(jnp.where(masked[..., None], grad_start, 0.0), axis=(0, 1))
    grad_input = jnp.where(masked[..., None], 0.0, grad_start)
    grad_mod = jnp.concatenate(
        [
            grad_shift_one,
            grad_scale_one,
            grad_gate_one,
            grad_shift_two,
            grad_scale_two,
            grad_gate_two,
        ],
        axis=1,
    )
    grad_w_ada = jnp.dot(cond_bf.astype(jnp.float32).T, grad_mod, precision=lax.Precision.HIGHEST)
    grad_vectors = jnp.concatenate(
        [
            grad_gain_one[None, :],
            grad_gain_two[None, :],
            jnp.sum(grad_mod, axis=0).reshape(6, width),
            grad_mask_row[None, :],
        ],
        axis=0,
    )
    red_ada, red_qkv, red_attn, red_in, red_out, red_vec = (
        lax.psum_scatter(grad_w_ada, ("dp", "seq"), scatter_dimension=1, tiled=True),
        lax.psum_scatter(grad_w_qkv, ("dp", "seq"), scatter_dimension=0, tiled=True),
        lax.psum_scatter(grad_w_attn, ("dp", "seq"), scatter_dimension=0, tiled=True),
        lax.psum_scatter(grad_w_in, ("dp", "seq"), scatter_dimension=0, tiled=True),
        lax.psum_scatter(grad_w_out, ("dp", "seq"), scatter_dimension=0, tiled=True),
        lax.psum_scatter(grad_vectors, ("dp", "seq"), scatter_dimension=1, tiled=True),
    )
    local_squares = jnp.float32(0.0)
    for reduced in (red_vec, red_ada, red_qkv, red_attn, red_in, red_out):
        local_squares = local_squares + jnp.sum(reduced * reduced)
    grad_norm = jnp.sqrt(lax.psum(local_squares, ("dp", "seq")))
    clip_factor = jnp.minimum(1.0, CLIP / (grad_norm + 1e-06))
    columns = red_vec.shape[1]
    own_vectors = lax.dynamic_slice_in_dim(
        vectors, lax.axis_index(("dp", "seq")) * columns, columns, 1
    )
    vec_out = adam_step(own_vectors, red_vec * clip_factor, m_vec, v_vec, RATE_VECTORS, 0.0)
    ada_out = adam_step(w_ada, red_ada * clip_factor, m_ada, v_ada, RATE, DECAY)
    qkv_out = adam_step(w_qkv, red_qkv * clip_factor, m_qkv, v_qkv, RATE, DECAY)
    attn_out = adam_step(w_attn, red_attn * clip_factor, m_attn, v_attn, RATE, DECAY)
    in_out = adam_step(w_in, red_in * clip_factor, m_in, v_in, RATE, DECAY)
    out_out = adam_step(w_out, red_out * clip_factor, m_out, v_out, RATE, DECAY)
    return (
        block_out,
        grad_input,
        grad_norm,
        vec_out[0],
        vec_out[1],
        vec_out[2],
        ada_out[0],
        ada_out[1],
        ada_out[2],
        qkv_out[0],
        qkv_out[1],
        qkv_out[2],
        attn_out[0],
        attn_out[1],
        attn_out[2],
        in_out[0],
        in_out[1],
        in_out[2],
        out_out[0],
        out_out[1],
        out_out[2],
    )


F32, BF = jnp.float32, jnp.bfloat16
MESH = pl.DeviceIdType.MESH
DP, LINE, SEQ, CHIPS, ALL = 4, 4, 8, 16, 32
ROWS, WIDTH, PACK = 128, 768, 640
HALF = WIDTH // 2
HALVES = ((0, 0), (0, 1), (0, 2), (2, 2), (1, 0), (1, 1), (1, 2), None, (2, 0), (2, 1))

def numbered(**counts):
    at = {}
    for name, count in counts.items():
        at[name] = sum(counts[other] for other in at)
    return SimpleNamespace(**at), sum(counts.values())


S, SEM_COUNT = numbered(
    load=11,
    cond=1,
    mix_qkv=1,
    mix_in=1,
    mix_attn=1,
    mod=1,
    w_qkv=1,
    w_attn=1,
    plane_in=1,
    w_in=4,
    w_out=4,
    group_qkv=4,
    group_attn=4,
    fw_qkv=1,
    fw_attn=1,
    fw_in=1,
    fw_out=1,
    tok=4,
    h2=4,
    dm=4,
    xf=4,
    o=1,
    mm=1,
    dh2=1,
    do=1,
    gp=1,
    dh1=5,
    pair_out=1,
    pair_in=1,
    pair_attn=1,
    pair_qkv=1,
    plane_attn=1,
    plane_qkv=1,
    line_out=5,
    line_in=5,
    slice_in=1,
    line_attn=1,
    line_qkv=1,
    last_in=1,
    last_attn=1,
    last_qkv=1,
    early=1,
    early2=1,
    late=1,
    late2=1,
    sq=1,
)

SCRATCH = dict(
    i_tok=((1, 128, 768), BF),
    i_cot=((1, 128, 768), BF),
    i_vec=((9, 768), F32),
    i_wada=((144, 128), F32),
    i_wqkv=((24, 2304), F32),
    i_wattn=((24, 768), F32),
    i_win=((24, 3072), F32),
    i_wout=((96, 768), F32),
    wide_qkv=((48, 3072), F32),
    wide_in=((48, 3072), F32),
    wide_attn=((48, 768), F32),
    s_qkv=((48, 3072), BF),
    s_in=((48, 3072), BF),
    s_attn=((48, 768), BF),
    w_qkv=((768, 768), BF),
    w_in=((4, 4, 48, 768), BF),
    w_attn=((768, 768), BF),
    w_out=((4, 2, 96, 768), BF),
    conds_all=((4, 8, 128), F32),
    mod_send=((4, 4, 128), F32),
    mod_got=((32, 4, 128), F32),
    mod_flat=((40, 128), F32),
    mod_pad=((8, 384), F32),
    turn=((2, 4, 128, 128), F32),
    dmod_flat=((4, 40, 128), F32),
    mod=((8, 768), F32),
    x0=((128, 768), F32),
    n1=((128, 768), F32),
    inv1=((128, 128), F32),
    x1=((128, 768), F32),
    n2=((128, 768), F32),
    inv2=((128, 128), F32),
    a=((128, 768), F32),
    dx1=((128, 768), F32),
    toks=((4, 128, 768), BF),
    h1=((4, 128, 768), BF),
    h2=((4, 128, 768), BF),
    dm=((4, 128, 768), BF),
    gb=((4, 128, 768), BF),
    du=((4, 128, 768), BF),
    xb=((2, 4, 128, 640), BF),
    pt=((3, 1024, 512), BF),
    vt=((2, 128, 1024), BF),
    kt=((2, 128, 1024), BF),
    back=((4, 128, 768), F32),
    ot=((2, 128, 512), F32),
    os=((4, 192, 128), BF),
    ob=((4, 192, 128), BF),
    o2=((4, 128, 128), BF),
    mms=((4, 128, 768), BF),
    mmr=((4, 128, 768), BF),
    dhs=((4, 128, 768), BF),
    dhr=((4, 128, 768), BF),
    das=((128, 768), BF),
    dos=((4, 192, 128), BF),
    dob=((4, 192, 128), BF),
    dst=((3, 1024, 512), BF),
    ga=((512, 640), F32),
    gps=((512, 512), BF),
    gpr=((512, 512), BF),
    dqkv=((4, 128, 768), BF),
    d1s=((4, 128, 768), BF),
    d1r=((4, 128, 768), BF),
    g_out=((4, 2, 96, 768), BF),
    g_in=((2, 4, 4, 48, 384), BF),
    g_attn=((2, 768, 384), BF),
    g_qkv=((2, 768, 384), BF),
    p_out=((4, 96, 768), BF),
    p_in=((4, 4, 48, 384), BF),
    p_attn=((768, 384), BF),
    p_qkv=((768, 384), BF),
    q_attn=((4, 192, 384), BF),
    q_qkv=((4, 192, 384), BF),
    m_attn=((192, 384), BF),
    m_qkv=((192, 384), BF),
    r_out=((4, 96, 768), BF),
    r_in=((4, 4, 48, 384), BF),
    via_in=((4, 48, 384), BF),
    via_out=((96, 768), BF),
    via_dh1=((128, 768), BF),
    m_in=((4, 48, 384), BF),
    u_in=((4, 48, 384), BF),
    r_attn=((4, 48, 384), BF),
    r_qkv=((4, 48, 384), BF),
    t_in=((4, 48, 384), F32),
    t_attn=((1, 48, 384), F32),
    t_qkv=((4, 48, 384), F32),
    f_in=((4, 2, 24, 384), F32),
    f_attn=((1, 2, 24, 384), F32),
    f_qkv=((4, 2, 24, 384), F32),
    early=((8, 768), F32),
    early_got=((8, 8, 768), F32),
    early_all=((4, 8, 768), F32),
    late=((4, 768), F32),
    late_got=((8, 4, 768), F32),
    late_all=((4, 4, 768), F32),
    sq=((32, 1, 128), F32),
)


def dot(left, right):
    return jnp.dot(left, right, preferred_element_type=F32)


def dot_nt(left, right):
    return lax.dot_general(left, right, (((1,), (1,)), ((), ())), preferred_element_type=F32)


def dot_tn(left, right):
    return lax.dot_general(left, right, (((0,), (0,)), ((), ())), preferred_element_type=F32)


def loop(count, body, start=0):
    def step(index, carry):
        body(index)
        return carry

    lax.fori_loop(start, count, step, 0)


def layer_kernel(
    i_time,
    i_start,
    i_len,
    h_tok,
    h_cot,
    h_vec,
    h_wada,
    h_wqkv,
    h_wattn,
    h_win,
    h_wout,
    o_y,
    o_dx,
    o_norm,
    o_gqkv,
    o_gattn,
    o_gin,
    o_gout,
    o_dmod,
    o_gvec,
    o_vec,
    o_conds,
    *scratch,
):
    r = SimpleNamespace(**dict(zip(SCRATCH, scratch)), when=scratch[-3])
    send_sems, recv_sems = scratch[-2:]
    i_tok, i_cot, i_vec, i_wada = r.i_tok, r.i_cot, r.i_vec, r.i_wada
    i_wqkv, i_wattn, i_win, i_wout = r.i_wqkv, r.i_wattn, r.i_win, r.i_wout
    b, s = lax.axis_index("dp"), lax.axis_index("seq")
    z, c = lax.div(s, 2), lax.rem(s, 2)
    mate = s + 1 - 2 * c
    chip = b * LINE + z
    me = b * SEQ + s
    drains = []

    def push(src, dst, at, to_b, to_s, out=None):
        pltpu.make_async_remote_copy(
            src_ref=src,
            dst_ref=dst,
            send_sem=send_sems.at[at if out is None else out],
            recv_sem=recv_sems.at[at],
            device_id=(to_b, to_s),
            device_id_type=MESH,
        ).start()

    def keep(src, dst, at):
        pltpu.make_async_copy(src, dst, recv_sems.at[at]).start()

    def got(at, like):
        pltpu.make_async_copy(like, like, recv_sems.at[at]).wait()

    def left(at, like):
        pltpu.make_async_copy(like, like, send_sems.at[at]).wait()

    def sent(at, like):
        drains.append((at, like))

    near = (b, b + 1 - 2 * lax.rem(b, 2), b + 2 - 4 * lax.div(b, 2), 3 - b)

    def peers(body):
        for k in (1, 2, 3):
            body(k, near[k])

    def stack(body):
        for k in (1, 2, 3):
            body(lax.rem(z + k, LINE))

    def line_gather(block, at, near=True, rest=True):
        inner = 1 + lax.rem(z, 2)
        if near:
            push(block(z), block(z), at + z, b, 2 * inner + c, at)

        def one(to):
            relayed = ((z == 1) & (to == 3)) | ((z == 2) & (to == 0))

            @pl.when(jnp.logical_not(relayed | (to == inner)))
            def _():
                push(block(z), block(z), at + z, b, 2 * to + c, at)

        if rest:
            stack(one)

    def line_relay(block, at):
        for middle, source, to in ((2, 1, 3), (1, 2, 0)):

            @pl.when(z == middle)
            def _():
                got(at + source, block(source))
                push(block(source), block(source), at + source, b, 2 * to + c, at)

    def line_got(block, at, k):
        here = (k == z) | ((z == 2) & (k == 1)) | ((z == 1) & (k == 2))

        @pl.when(jnp.logical_not(here))
        def _():
            got(at + k, block(0))

    far = lax.div(z, 2)

    def line_order(j):
        return lax.rem(z + (2, 3 - 2 * far, 1 + 2 * far, 0)[j], LINE)

    def line_add(j, rows, dst, via, at):
        to = line_order(j)
        outer_chip = (z == 0) | (z == 3)

        def direct():
            push(rows(to), dst.at[z], at + z, b, 2 * to + c, at)

        if j == 0:

            @pl.when(outer_chip)
            def _():
                push(rows(to), via, at + 4, b, 2 * (1 + far) + c, at)

            @pl.when(jnp.logical_not(outer_chip))
            def _():
                direct()

        elif j < 3:
            direct()
        else:
            keep(rows(z), dst.at[z], at + z)

    def line_via(via, at, add):
        @pl.when((z == 1) | (z == 2))
        def _():
            got(at + 4, via)
            add()

    def line_done(dst, at):
        for k in range(4):
            missing = ((z == 1) & (k == 3)) | ((z == 2) & (k == 0))

            @pl.when(jnp.logical_not(missing))
            def _():
                got(at + k, dst.at[k])

    def line_clear(dst):
        for middle, k in ((1, 3), (2, 0)):

            @pl.when(z == middle)
            def _():
                dst[k] = jnp.zeros(dst.shape[1:], BF)

    lane = lax.broadcasted_iota(jnp.int32, (1, 128), 1)
    low = lane < 64
    own24 = pl.ds(pl.multiple_of(24 * c, 8), 24)
    mate24 = pl.ds(pl.multiple_of(24 * (1 - c), 8), 24)
    part = pl.ds(pl.multiple_of(HALF * c, 128), HALF)
    chip_rows = pl.ds(pl.multiple_of(48 * chip, 16), 48)
    group_rows = pl.ds(pl.multiple_of(192 * b, 16), 192)

    barrier = pltpu.get_barrier_semaphore()

    def greet(k):
        other = lax.rem(me + k, ALL)
        pl.semaphore_signal(
            barrier, inc=1, device_id=(lax.div(other, SEQ), lax.rem(other, SEQ)), device_id_type=MESH
        )

    loads = (
        (i_time, r.when.at[0]),
        (i_start, r.when.at[1]),
        (i_len, r.when.at[2]),
        (h_wqkv, i_wqkv),
        (h_win, i_win),
        (h_wattn, i_wattn),
        (h_wout, i_wout),
        (h_tok, i_tok),
        (h_vec, i_vec),
        (h_wada, i_wada),
        (h_cot, i_cot),
    )
    for k, (src, dst) in enumerate(loads):
        pltpu.make_async_copy(src, dst, recv_sems.at[S.load + k]).start()
    loop(ALL, greet, 1)
    for k, (src, dst) in enumerate(loads):
        pltpu.make_async_copy(src, dst, recv_sems.at[S.load + k]).wait()

    def natural(kind, p, head):
        return kind * WIDTH + 192 * p + 64 * head

    def half_at(ref, column, high):
        tile = ref[:, column // 128 * 128 : column // 128 * 128 + 128]
        return tile if (column % 128 == 64) == high else pltpu.roll(tile, 64, 1)

    for p in range(4):
        for tile in range(5):
            pair = []
            for high in (0, 1):
                which = HALVES[2 * tile + high]
                pair.append(
                    jnp.zeros((24, 128), F32)
                    if which is None
                    else half_at(i_wqkv, natural(which[0], p, which[1]), bool(high))
                )
            r.wide_qkv[own24, 768 * p + 128 * tile : 768 * p + 128 * tile + 128] = jnp.where(
                low, pair[0], pair[1]
            )
        r.wide_qkv[own24, 768 * p + 640 : 768 * p + 768] = jnp.zeros((24, 128), F32)
    r.wide_in[own24, :] = i_win[...]
    r.wide_attn[own24, :] = i_wattn[...]
    r.w_out[z, c] = i_wout[...].astype(BF)
    r.toks[z] = i_tok[0]
    line_clear(r.r_out)
    line_clear(r.r_in)
    line_clear(r.d1r)
    lanes8 = lax.broadcasted_iota(jnp.int32, (8, 128), 1)
    half_cond = COND // 2
    speed = jnp.exp((lanes8 % half_cond).astype(F32) * (-math.log(10000.0) / half_cond))
    angle = r.when[0, 0].astype(F32) * speed
    wave = jnp.where(lanes8 < half_cond, jnp.cos(angle), jnp.sin(angle))
    r.conds_all[b] = wave * (1.0 / (1.0 + jnp.exp(-wave)))
    pl.semaphore_wait(barrier, ALL - 1)

    def token_block(k):
        return r.toks.at[k]

    def in_block(k):
        return r.w_in.at[:, k, :, part]

    def out_block(k):
        return r.w_out.at[k, c]

    peers(lambda k, to: push(r.conds_all.at[b], r.conds_all.at[b], S.cond, to, s))
    sent(S.cond, r.conds_all.at[0:3])
    push(r.wide_qkv.at[own24], r.wide_qkv.at[own24], S.mix_qkv, b, mate)
    sent(S.mix_qkv, r.wide_qkv.at[0:24])
    push(r.wide_attn.at[own24], r.wide_attn.at[own24], S.mix_attn, b, mate)
    sent(S.mix_attn, r.wide_attn.at[0:24])
    push(r.wide_in.at[own24], r.wide_in.at[own24], S.mix_in, b, mate)
    sent(S.mix_in, r.wide_in.at[0:24])

    line_gather(token_block, S.tok, rest=False)
    sent(S.tok, r.toks.at[0:3])

    got(S.cond, r.conds_all.at[0:3])
    row8 = lax.broadcasted_iota(jnp.int32, (8, 128), 0)
    cond4 = jnp.zeros((8, 128), F32)
    for k in range(4):
        cond4 = jnp.where(row8 == k, r.conds_all[k], cond4)
    o_conds[...] = cond4
    wide = i_wada.shape[0]
    r.mod_pad[...] = jnp.zeros((8, 384), F32)
    r.mod_pad[:, 0:wide] = dot_nt(cond4.astype(BF), i_wada[...].astype(BF))
    columns = pltpu.roll(r.mod_pad[...], lax.rem(wide * me, 128), 1)
    for k in range(4):
        for t in range(3):
            r.mod_send[k, t : t + 1, :] = columns[k : k + 1, 128 * t : 128 * t + 128]
        r.mod_send[k, 3:4, :] = jnp.zeros((1, 128), F32)

    def send_mod(k):
        other = lax.rem(me + k, ALL)
        ob = lax.div(other, SEQ)
        push(r.mod_send.at[ob], r.mod_got.at[me], S.mod, ob, lax.rem(other, SEQ))

    loop(ALL, send_mod, 1)
    sent(S.mod, r.mod_got.at[0:31])
    keep(r.mod_send.at[b], r.mod_got.at[me], S.mod)

    def block(src, first):
        return src.at[:, pl.ds(pl.multiple_of(first, 128), HALF)]

    def along_line(src, dst, at, step):
        stack(
            lambda to: push(
                block(src, step * to + HALF * c), dst.at[chip_rows, part], at, b, 2 * to + c
            )
        )
        keep(block(src, step * z + HALF * c), dst.at[chip_rows, part], at)
        sent(at, dst.at[0:144, 0:HALF])

    def over_plane(dst, first, at):
        got(first, dst.at[0:192, 0:HALF])
        rows = dst.at[group_rows, part]
        for k in (1, 2, 3):
            push(rows, rows, at + k, near[k], s)
            sent(at + k, dst.at[0:192, 0:HALF])

    def share(dst, at, onward):
        for k in range(4):
            rows = dst.at[pl.ds(pl.multiple_of(192 * near[k], 16), 192), part]
            if k:
                got(at + k, rows)
            push(rows, rows, onward, b, mate)
        sent(onward, dst.at[:, 0:HALF])

    def line_share(block, at, onward):
        for k in range(4):
            line_got(block, at, k)
            push(block(k), block(k), onward, b, mate)

    got(S.mix_qkv, r.wide_qkv.at[0:24])
    r.s_qkv[...] = r.wide_qkv[...].astype(BF)
    along_line(r.s_qkv, r.w_qkv, S.w_qkv, WIDTH)
    got(S.mix_attn, r.wide_attn.at[0:24])
    r.s_attn[...] = r.wide_attn[...].astype(BF)
    over_plane(r.w_qkv, S.w_qkv, S.group_qkv)
    line_gather(token_block, S.tok, near=False)
    along_line(r.s_attn, r.w_attn, S.w_attn, 0)
    line_gather(out_block, S.w_out)
    sent(S.w_out, r.w_out.at[0:3, 0])
    got(S.mix_in, r.wide_in.at[0:24])
    r.s_in[...] = r.wide_in[...].astype(BF)
    peers(
        lambda k, to: push(
            block(r.s_in, WIDTH * to + HALF * c), r.w_in.at[b, z, :, part], S.plane_in, to, s
        )
    )
    keep(block(r.s_in, WIDTH * b + HALF * c), r.w_in.at[b, z, :, part], S.plane_in)
    sent(S.plane_in, r.w_in.at[0:3, 0, :, 0:HALF])

    def start_tokens(tokens, k):
        place = (2 * k + c) * ROWS + lax.broadcasted_iota(jnp.int32, (ROWS, 1), 0)
        hidden = (place >= r.when[1, 0]) & (place < r.when[1, 0] + r.when[2, 0])
        return jnp.where(hidden, i_vec[8:9, :], tokens.astype(F32)), hidden

    x0, _ = start_tokens(i_tok[0], z)
    r.x0[...] = x0
    n1, inv1 = normalize(x0)
    r.n1[...] = n1
    r.inv1[...] = jnp.broadcast_to(inv1, (ROWS, 128))

    got(S.mod, r.mod_got)
    r.mod_flat[...] = jnp.zeros((40, 128), F32)
    for k in range(ALL):
        first = 9 * k // 8
        r.mod_flat[first : first + 3, :] += r.mod_got[k, 0:3, :]
    for k in range(6):
        row = jnp.concatenate(
            [r.mod_flat[6 * k + t : 6 * k + t + 1, :] for t in range(6)], axis=1
        )
        r.mod[k : k + 1, :] = row + i_vec[2 + k : 3 + k, :]

    def mod(k):
        return r.mod[k : k + 1, :]

    def vec(k):
        return i_vec[k : k + 1, :]

    r.h1[z] = (r.n1[...] * vec(0) * (1.0 + mod(1)) + mod(0)).astype(BF)
    r.dm[0] = (i_cot[0].astype(F32) * mod(5)).astype(BF)
    peers(lambda k, to: push(r.dm.at[0], r.dm.at[k], S.dm + k, to, s))
    for k in (1, 2, 3):
        sent(S.dm + k, r.dm.at[0])

    lanes = lax.broadcasted_iota(jnp.int32, (ROWS, 128), 1)
    first_half = lanes % HD < HD // 2
    speed = jnp.exp((lanes % (HD // 2)).astype(F32) * (-math.log(10000.0) / (HD // 2)))
    row = lax.broadcasted_iota(jnp.int32, (ROWS, 128), 0)

    def table(k):
        angle = ((2 * k + c) * ROWS + row).astype(F32) * speed
        r.turn[0, k] = jnp.cos(angle)
        sine = jnp.sin(angle)
        r.turn[1, k] = jnp.where(first_half, -sine, sine)

    loop(LINE, table)

    line_relay(token_block, S.tok)

    share(r.w_qkv, S.group_qkv, S.fw_qkv)
    got(S.fw_qkv, r.w_qkv.at[:, 0:HALF])

    def turned(tile, sign, k):
        other = jnp.where(first_half, pltpu.roll(tile, 96, 1), pltpu.roll(tile, 32, 1))
        return tile * r.turn[0, k] + sign * (other * r.turn[1, k])

    def project(j):
        k = lax.rem(z + j, LINE)

        @pl.when(j > 0)
        def _():
            line_got(token_block, S.tok, k)
            other, _ = start_tokens(r.toks[k], k)
            other, _ = normalize(other)
            r.h1[k] = (other * vec(0) * (1.0 + mod(1)) + mod(0)).astype(BF)

        x = dot(r.h1[k], r.w_qkv[:, 0:PACK])
        tiles = [x[:, 128 * t : 128 * t + 128] for t in range(5)]
        tiles[0] = turned(tiles[0], 1.0, k) * 0.125
        tiles[1] = jnp.where(low, turned(tiles[1], 1.0, k) * 0.125, tiles[1])
        tiles[2] = turned(tiles[2], 1.0, k)
        tiles[3] = turned(tiles[3], 1.0, k)
        for t in range(5):
            r.xb[0, k, :, 128 * t : 128 * t + 128] = tiles[t].astype(BF)
        push(r.xb.at[0, k], r.xb.at[1, k], S.xf + k, b, mate)

    loop(4, project)
    over_plane(r.w_attn, S.w_attn, S.group_attn)
    for k in range(4):
        sent(S.xf + k, r.xb.at[0, 0])

    for k in range(4):
        got(S.xf + k, r.xb.at[0, 0])

    def tile_of(t):
        return r.xb[:, :, :, 128 * t : 128 * t + 128].reshape(1024, 128)

    heads = ((0, 2, 4, True, True), (0, 2, 4, False, False), (1, 3, 1, True, False))

    def queries(head, first, size):
        q_tile, _, _, q_low, _ = heads[head]
        q = r.xb[0, first : first + size, :, 128 * q_tile : 128 * q_tile + 128]
        return jnp.where(low if q_low else ~low, q.reshape(size * 128, 128), jnp.zeros((), BF))

    r.vt[0] = tile_of(4).T
    r.vt[1] = tile_of(1).T
    for half in range(2):
        at = slice(256 * half, 256 * half + 256)
        for head in range(3):
            scores = dot_nt(tile_of(heads[head][1]), queries(head, 2 * half, 2))
            weights = jnp.exp(scores - jnp.max(scores, axis=0, keepdims=True))
            weights = weights * (1.0 / jnp.sum(weights, axis=0, keepdims=True))
            weights = weights.astype(BF)
            r.pt[head, :, at] = weights
            out = dot(r.vt[head // 2], weights)
            if head == 0:
                r.ot[0, 0:64, at] = out[0:64]
            elif head == 1:
                r.ot[0, 64:128, at] = out[64:128]
            else:
                r.ot[1, 0:64, at] = out[64:128]
                r.ot[1, 64:128, at] = jnp.zeros((64, 256), F32)
        for k in (2 * half, 2 * half + 1):
            across = slice(128 * k, 128 * k + 128)
            r.os[k, 0:128, :] = r.ot[0, :, across].T.astype(BF)
            third = r.ot[1, 0:64, across]
            third = jnp.concatenate([third, pltpu.roll(third, 64, 1)], axis=0)
            r.os[k, 128:192, :] = third.T[0:64].astype(BF)
        for to in (2 * half, 2 * half + 1):

            @pl.when(z == to)
            def _():
                keep(r.os.at[to], r.ob.at[z], S.o)

            @pl.when(z != to)
            def _():
                push(r.os.at[to], r.ob.at[z], S.o, b, 2 * to + c)

        if half == 0:
            line_relay(out_block, S.w_out)

    sent(S.o, r.os.at[0:3])
    got(S.plane_in, r.w_in.at[:, 0, :, 0:HALF])
    line_gather(in_block, S.w_in)
    sent(S.w_in, r.w_in.at[0:3, :, :, 0:HALF])
    for k in range(2):
        r.kt[k] = tile_of(2 + k).T
    share(r.w_attn, S.group_attn, S.fw_attn)
    got(S.fw_attn, r.w_attn.at[:, 0:HALF])
    got(S.o, r.ob)
    a = jnp.zeros((ROWS, WIDTH), F32)
    for p in range(4):
        third = r.ob[p, 128:192, :].astype(F32)
        third = jnp.concatenate([third, pltpu.roll(third, 64, 1)], axis=0)
        r.o2[p] = jnp.where(low, third, 0.0).astype(BF)
        a += dot(r.ob[p, 0:128, :], r.w_attn[192 * p : 192 * p + 128, :])
        a += dot(r.o2[p, :, 0:64], r.w_attn[192 * p + 128 : 192 * p + 192, :])
    r.a[...] = a
    x1 = r.x0[...] + mod(2) * a
    r.x1[...] = x1
    n2, inv2 = normalize(x1)
    r.n2[...] = n2
    r.inv2[...] = jnp.broadcast_to(inv2, (ROWS, 128))
    r.h2[0] = (n2 * vec(1) * (1.0 + mod(4)) + mod(3)).astype(BF)
    peers(lambda k, to: push(r.h2.at[0], r.h2.at[k], S.h2 + k, to, s))
    for k in (1, 2, 3):
        sent(S.h2 + k, r.h2.at[0])
    line_relay(in_block, S.w_in)
    line_share(out_block, S.w_out, S.fw_out)
    sent(S.fw_out, r.w_out.at[:, 0])
    got(S.fw_out, r.w_out.at[:, 0])

    def feed_back(k):
        @pl.when(k > 0)
        def _():
            got(S.dm + k, r.dm.at[0])

        r.back[k] = dot_nt(r.dm[k], r.w_out[...].reshape(WIDTH, WIDTH))

    loop(4, feed_back)
    line_share(in_block, S.w_in, S.fw_in)
    sent(S.fw_in, r.w_in.at[:, :, :, 0:HALF])
    got(S.fw_in, r.w_in.at[:, :, :, 0:HALF])

    def feed(first, count):
        at = slice(first, first + count)
        size = count * ROWS
        u = dot(r.h2[at].reshape(size, WIDTH), r.w_in[...].reshape(WIDTH, WIDTH))
        slope = 0.7978845608028654
        cube = 0.044715
        t = jnp.tanh(slope * (u + cube * u * u * u))
        r.gb[at] = (0.5 * u * (1.0 + t)).astype(BF).reshape(count, ROWS, WIDTH)
        bend = 0.5 * (1.0 + t) + 0.5 * u * (1.0 - t * t) * (slope * (1.0 + 3.0 * cube * u * u))
        du = (r.back[at].reshape(size, WIDTH) * bend).astype(BF)
        r.du[at] = du.reshape(count, ROWS, WIDTH)
        r.dhs[at] = dot_nt(du, r.w_in[...].reshape(WIDTH, WIDTH)).astype(BF).reshape(count, ROWS, WIDTH)

    feed(0, 1)
    for first, count in ((1, 2), (3, 1)):
        for k in range(first, first + count):
            got(S.h2 + k, r.h2.at[0])
        feed(first, count)
        for k in range(first, first + count):
            push(r.dhs.at[k], r.dhr.at[k], S.dh2, near[k], s)
    sent(S.dh2, r.dhs.at[0:3])
    def gather(own, others):
        total = own[0].astype(F32)
        for k in (1, 2, 3):
            total += others[k].astype(F32)
        return total

    for k in range(2):
        rows = slice(384 * k, 384 * k + 384)
        result = dot_tn(r.gb[:, :, rows].reshape(512, 384), r.dm[...].reshape(512, 768))
        r.g_out[2 * k : 2 * k + 2] = result.astype(BF).reshape(2, 2, 96, 768)
    push(r.g_out.at[:, 1 - c], r.p_out, S.pair_out, b, mate)
    sent(S.pair_out, r.p_out)

    def outer(left, right, dst):
        for k in range(2):
            rows = slice(384 * k, 384 * k + 384)
            result = dot_tn(
                left[:, :, rows].reshape(512, 384), right[...].reshape(512, 768)
            ).astype(BF)
            dst[0, rows, :] = result[:, 0:HALF]
            dst[1, rows, :] = result[:, HALF:WIDTH]

    def to_mate(grad, dst, at):
        push(grad.at[1 - c], dst, at, b, mate)
        sent(at, dst)

    def pair_sum(grad, pair, at):
        got(at, pair)
        grad[c] = (grad[c].astype(F32) + pair[...].astype(F32)).astype(BF)

    def plane_sum(grad, dst, at):
        def rows(to):
            return grad.at[c, pl.ds(pl.multiple_of(192 * to, 16), 192)]

        peers(lambda k, to: push(rows(to), dst.at[k], at, to, s))
        keep(rows(b), dst.at[0], at)
        sent(at, dst.at[0:3])

    def line_sum(src, total, dst, first, at):
        got(first, src)
        total[...] = (
            (src[0].astype(F32) + src[1].astype(F32)) + (src[2].astype(F32) + src[3].astype(F32))
        ).astype(BF)

        def rows(to):
            return total.at[pl.ds(pl.multiple_of(48 * to, 16), 48)]

        stack(lambda to: push(rows(to), dst.at[z], at, b, 2 * to + c))
        keep(rows(z), dst.at[z], at)
        sent(at, dst.at[0:3])

    def trade(total, final, at):
        push(total.at[:, mate24], final.at[:, c], at, b, mate)
        sent(at, final.at[:, 0])
        final[:, c] = total[:, own24, :]

    for k in range(2):
        rows = slice(384 * k, 384 * k + 384)
        result = dot_tn(r.h2[:, :, rows].reshape(512, 384), r.du[...].reshape(512, 768)).astype(BF)
        for h in range(2):
            r.g_in[h, 2 * k : 2 * k + 2] = result[:, 384 * h : 384 * h + 384].reshape(2, 4, 48, 384)
    to_mate(r.g_in, r.p_in, S.pair_in)

    got(S.pair_out, r.p_out)
    for k in range(4):
        r.g_out[k, c] = (r.g_out[k, c].astype(F32) + r.p_out[k].astype(F32)).astype(BF)

    def out_rows(k):
        return r.g_out.at[k, c]

    for j in (0, 1):
        line_add(j, out_rows, r.r_out, r.via_out, S.line_out)

    def add_out():
        k = line_order(2)
        r.g_out[k, c] = (r.g_out[k, c].astype(F32) + r.via_out[...].astype(F32)).astype(BF)

    got(S.dh2, r.dhr.at[0:3])
    dh = gather(r.dhs, r.dhr)
    n2 = r.n2[...]
    inv2 = r.inv2[:, 0:1]
    r.early[...] = jnp.zeros((8, 768), F32)
    r.early[2:3, :] = jnp.sum(dh, axis=0, keepdims=True)
    both = jnp.sum(dh * n2, axis=0, keepdims=True)
    r.early[3:4, :] = both * vec(1)
    r.early[0:1, :] = both * (1.0 + mod(4))
    grad = dh * ((1.0 + mod(4)) * vec(1))
    dx1 = i_cot[0].astype(F32) + norm_back(n2, inv2, grad)
    r.dx1[...] = dx1
    r.early[1:2, :] = jnp.sum(dx1 * r.a[...], axis=0, keepdims=True)
    r.das[...] = (dx1 * mod(2)).astype(BF)
    for p in range(4):
        first = 192 * p
        r.dos[p, 0:128, :] = dot_nt(r.das[...], r.w_attn[first : first + 128, :]).astype(BF)
        tail = dot_nt(r.das[...], r.w_attn[first + 128 : first + 192, :])
        tail = jnp.concatenate([tail, jnp.zeros((ROWS, 64), F32)], axis=1)
        r.dos[p, 128:192, :] = jnp.where(low, tail[0:64], pltpu.roll(tail[64:128], 64, 1)).astype(
            BF
        )

    stack(lambda to: push(r.dos.at[to], r.dob.at[z], S.do, b, 2 * to + c))
    keep(r.dos.at[z], r.dob.at[z], S.do)
    sent(S.do, r.dos.at[0:3])
    for t in range(3):
        at = slice(256 * t, 256 * t + 256)
        mm = dot(r.gb[...].reshape(512, WIDTH), r.w_out[:, :, :, at].reshape(WIDTH, 256))
        r.mms[:, :, at] = mm.astype(BF).reshape(4, ROWS, 256)
    peers(lambda k, to: push(r.mms.at[k], r.mmr.at[k], S.mm, to, s))
    sent(S.mm, r.mms.at[0:3])

    for p in range(4):
        for rows, left_side in (
            (slice(192 * p, 192 * p + 128), r.ob[p, 0:128, :]),
            (slice(192 * p + 128, 192 * p + 192), r.o2[p]),
        ):
            result = dot_tn(left_side, r.das[...])[0 : rows.stop - rows.start].astype(BF)
            r.g_attn[0, rows, :] = result[:, 0:HALF]
            r.g_attn[1, rows, :] = result[:, HALF:WIDTH]
    to_mate(r.g_attn, r.p_attn, S.pair_attn)

    def over_line(src, dst, name):
        def one(k):
            push(src, dst.at[s], name, b, lax.rem(s + k, SEQ))

        loop(SEQ, one, 1)
        keep(src, dst.at[s], name)
        sent(name, dst.at[0:7])

    def over_group(got_ref, dst, name):
        total = got_ref[0]
        for k in range(1, SEQ):
            total += got_ref[k]
        dst[b] = total
        peers(lambda k, to: push(dst.at[b], dst.at[b], name, to, s))
        sent(name, dst.at[0:3])


    pair_sum(r.g_in, r.p_in, S.pair_in)

    line_via(r.via_out, S.line_out, add_out)
    for j in (2, 3):
        line_add(j, out_rows, r.r_out, r.via_out, S.line_out)
    sent(S.line_out, r.r_out.at[0:3])

    def in_rows(k):
        return r.g_in.at[c, :, k]

    for j in (0, 1):
        line_add(j, in_rows, r.r_in, r.via_in, S.line_in)

    def add_in():
        k = line_order(2)
        r.g_in[c, :, k] = (r.g_in[c, :, k].astype(F32) + r.via_in[...].astype(F32)).astype(BF)

    pair_sum(r.g_attn, r.p_attn, S.pair_attn)
    plane_sum(r.g_attn, r.q_attn, S.plane_attn)

    got(S.do, r.dob)
    dot0 = r.dob[:, 0:128, :].reshape(512, 128)
    third = r.dob[:, 128:192, :].astype(F32).reshape(256, 128)
    other_rows = jnp.where(low, pltpu.roll(third, 64, 1), 0.0).reshape(4, 64, 128)
    third = jnp.where(low, third, 0.0).reshape(4, 64, 128)
    dot1 = jnp.concatenate([third, other_rows], axis=1).reshape(512, 128)
    zero = jnp.zeros((), BF)
    moved = pltpu.roll(dot1, 64, 1).astype(BF)
    grads = (jnp.where(low, dot0, zero), jnp.where(low, zero, dot0), moved)
    product = dot0.astype(F32).T * r.ot[0]
    deltas = (
        jnp.sum(product[0:64], axis=0, keepdims=True),
        jnp.sum(product[64:128], axis=0, keepdims=True),
        jnp.sum(dot1.T * r.ot[1], axis=0, keepdims=True),
    )
    for head in range(3):
        values = tile_of(heads[head][2])
        for half in range(2):
            at = slice(256 * half, 256 * half + 256)
            dp = dot_nt(values, grads[head][at])
            r.dst[head, :, at] = (
                r.pt[head, :, at].astype(F32) * (dp - deltas[head][:, at])
            ).astype(BF)

    def key_grads(rows):
        dk = [dot(r.dst[head, rows, :], queries(head, 0, 4)) for head in range(3)]
        dv = [dot(r.pt[head, rows, :], grads[head]) for head in range(3)]
        return (dv[2], dk[0] + dk[1], dk[2], dv[0] + dv[1])

    line_via(r.via_in, S.line_in, add_in)
    for j in (2, 3):
        line_add(j, in_rows, r.r_in, r.via_in, S.line_in)
    sent(S.line_in, r.r_in.at[0:3])
    for t, tile in enumerate(key_grads(slice(512, 1024))):
        r.gps[:, 128 * t : 128 * t + 128] = tile.astype(BF)
    push(r.gps, r.gpr, S.gp, b, mate)
    sent(S.gp, r.gps)
    for t, tile in enumerate(key_grads(slice(0, 512))):
        r.ga[:, 128 * t + 128 : 128 * t + 256] = tile
    for half in range(2):
        at = slice(256 * half, 256 * half + 256)
        turned_q = [dot(r.kt[head // 2], r.dst[head, :, at]) for head in range(3)]
        top = jnp.concatenate([turned_q[0][0:64], turned_q[1][64:128]], axis=0)
        r.ga[at, 0:128] = top.T * 0.125
        r.ga[at, 128:256] += turned_q[2].T * 0.125
    got(S.mm, r.mmr.at[0:3])
    mm = gather(r.mms, r.mmr)
    o_y[...] = (r.x1[...] + mod(5) * mm).astype(BF)
    r.early[4:5, :] = jnp.sum(i_cot[0].astype(F32) * mm, axis=0, keepdims=True)
    over_line(r.early, r.early_got, S.early)
    got(S.gp, r.gpr)

    def dh1_rows(k):
        return r.d1s.at[k]

    def back_turn(k):
        rows = pl.ds(pl.multiple_of(128 * k, 128), 128)
        tiles = [r.ga[rows, 0:128]] + [
            r.ga[rows, 128 * t : 128 * t + 128]
            + r.gpr[rows, 128 * t - 128 : 128 * t].astype(F32)
            for t in range(1, 5)
        ]
        tiles[0] = turned(tiles[0], -1.0, k)
        tiles[1] = jnp.where(low, turned(tiles[1], -1.0, k), tiles[1])
        tiles[2] = turned(tiles[2], -1.0, k)
        tiles[3] = turned(tiles[3], -1.0, k)
        for t in range(5):
            r.dqkv[k, :, 128 * t : 128 * t + 128] = tiles[t].astype(BF)
        r.dqkv[k, :, PACK:WIDTH] = jnp.zeros((128, 128), BF)

    loop(4, back_turn)

    def unproject(j):
        k = line_order(j)
        partial_sum = dot_nt(r.dqkv[k, :, 0:PACK], r.w_qkv[:, 0:PACK])
        r.d1s[k] = partial_sum.astype(BF)
        if j == 2:

            def add():
                r.d1s[k] = (partial_sum + r.via_dh1[...].astype(F32)).astype(BF)

            line_via(r.via_dh1, S.dh1, add)
        line_add(j, dh1_rows, r.d1r, r.via_dh1, S.dh1)

    unproject(0)
    outer(r.h1, r.dqkv, r.g_qkv)
    to_mate(r.g_qkv, r.p_qkv, S.pair_qkv)
    unproject(1)
    pair_sum(r.g_qkv, r.p_qkv, S.pair_qkv)
    plane_sum(r.g_qkv, r.q_qkv, S.plane_qkv)
    unproject(2)
    unproject(3)
    sent(S.dh1, r.d1s.at[0:3])
    line_sum(r.q_attn, r.m_attn, r.r_attn, S.plane_attn, S.line_attn)
    got(S.early, r.early_got)
    over_group(r.early_got, r.early_all, S.early2)

    line_done(r.r_in, S.line_in)
    r.m_in[...] = (
        (r.r_in[0].astype(F32) + r.r_in[1].astype(F32))
        + (r.r_in[2].astype(F32) + r.r_in[3].astype(F32))
    ).astype(BF)
    peers(lambda k, to: push(r.m_in.at[to], r.u_in.at[b], S.slice_in, to, s))
    keep(r.m_in.at[b], r.u_in.at[b], S.slice_in)
    sent(S.slice_in, r.u_in.at[0:3])
    line_sum(r.q_qkv, r.m_qkv, r.r_qkv, S.plane_qkv, S.line_qkv)

    line_done(r.d1r, S.dh1)
    dh = (r.d1r[0].astype(F32) + r.d1r[1].astype(F32)) + (
        r.d1r[2].astype(F32) + r.d1r[3].astype(F32)
    )
    n1 = r.n1[...]
    both = jnp.sum(dh * n1, axis=0, keepdims=True)
    r.late[0:1, :] = both * (1.0 + mod(1))
    r.late[1:2, :] = jnp.sum(dh, axis=0, keepdims=True)
    r.late[2:3, :] = both * vec(0)
    grad = dh * ((1.0 + mod(1)) * vec(0))
    dx0 = r.dx1[...] + norm_back(n1, r.inv1[:, 0:1], grad)
    _, hidden = start_tokens(i_tok[0], z)
    o_dx[...] = jnp.where(hidden, 0.0, dx0)
    r.late[3:4, :] = jnp.sum(jnp.where(hidden, dx0, 0.0), axis=0, keepdims=True)
    over_line(r.late, r.late_got, S.late)

    line_done(r.r_out, S.line_out)
    total = (r.r_out[0].astype(F32) + r.r_out[1].astype(F32)) + (
        r.r_out[2].astype(F32) + r.r_out[3].astype(F32)
    )
    o_gout[...] = total
    squares = total * total
    squares = jnp.sum(squares[:, 0:128] + squares[:, 128:256] + squares[:, 256:384]
                      + squares[:, 384:512] + squares[:, 512:640] + squares[:, 640:768],
                      axis=0, keepdims=True)

    def fold(value):
        total = value[:, 0:128] * value[:, 0:128]
        for t in range(1, value.shape[1] // 128):
            total += value[:, 128 * t : 128 * t + 128] * value[:, 128 * t : 128 * t + 128]
        return jnp.sum(total, axis=0, keepdims=True)

    got(S.slice_in, r.u_in)
    r.t_in[...] = r.u_in[...].astype(F32)
    for p in range(4):
        squares += fold(r.t_in[p])
    trade(r.t_in, r.f_in, S.last_in)
    got(S.line_attn, r.r_attn)
    r.t_attn[0] = (r.r_attn[0].astype(F32) + r.r_attn[1].astype(F32)) + (
        r.r_attn[2].astype(F32) + r.r_attn[3].astype(F32)
    )
    squares += fold(r.t_attn[0])
    trade(r.t_attn, r.f_attn, S.last_attn)
    got(S.line_qkv, r.r_qkv)
    r.t_qkv[...] = r.r_qkv[...].astype(F32)
    trade(r.t_qkv, r.f_qkv, S.last_qkv)
    for p in range(4):
        squares += fold(r.t_qkv[p])
    r.sq[me] = squares

    def send_sq(k):
        other = lax.rem(me + k, ALL)
        push(r.sq.at[me], r.sq.at[me], S.sq, lax.div(other, SEQ), lax.rem(other, SEQ))

    loop(ALL, send_sq, 1)
    sent(S.sq, r.sq.at[0:31])
    got(S.late, r.late_got)
    over_group(r.late_got, r.late_all, S.late2)
    got(S.last_in, r.f_in.at[:, 0])
    got(S.last_attn, r.f_attn.at[:, 0])
    for h in range(2):
        for p in range(4):
            value = r.f_in[p, h]
            o_gin[:, 768 * p + 384 * h : 768 * p + 384 * h + 384] = value
        value = r.f_attn[0, h]
        o_gattn[:, 384 * h : 384 * h + 384] = value
    got(S.last_qkv, r.f_qkv.at[:, 0])
    where = {which: index for index, which in enumerate(HALVES) if which is not None}

    def packed_half(chunk, high):
        kind, rest = chunk // 12, chunk % 12
        index = where[(kind, rest % 3)]
        t = index // 2
        tile = r.f_qkv[rest // 3, t // 3, :, t % 3 * 128 : t % 3 * 128 + 128]
        return tile if index % 2 == high else pltpu.roll(tile, 64, 1)

    for t in range(18):
        o_gqkv[:, 128 * t : 128 * t + 128] = jnp.where(
            low, packed_half(2 * t, 0), packed_half(2 * t + 1, 1)
        )
    got(S.early2, r.early_all.at[0:3])
    got(S.late2, r.late_all.at[0:3])
    mods = []
    for k in range(4):
        early, late = r.early_all[k], r.late_all[k]
        rows = jnp.concatenate([late[1:3], early[1:5], jnp.zeros((2, 768), F32)], axis=0)
        for n in range(6):
            for m in range(6):
                r.dmod_flat[k, 6 * n + m : 6 * n + m + 1, :] = rows[
                    n : n + 1, 128 * m : 128 * m + 128
                ]
        mods.append(rows)
    gain = jnp.concatenate(
        [
            sum(r.late_all[k][0:1] for k in range(4)),
            sum(r.early_all[k][0:1] for k in range(4)),
            (mods[0] + mods[1] + mods[2] + mods[3])[0:6],
        ],
        axis=0,
    )
    mask_row = sum(r.late_all[k][3:4] for k in range(4))
    gains = jnp.concatenate([gain, mask_row, jnp.zeros((7, 768), F32)], axis=0)
    masters = jnp.concatenate([i_vec[...], jnp.zeros((7, 768), F32)], axis=0)
    own = lax.rem(WIDTH - 24 * me, WIDTH)
    o_gvec[...] = pltpu.roll(gains, own, 1)[:, 0:128]
    o_vec[...] = pltpu.roll(masters, own, 1)[:, 0:128]
    r.mod_pad[...] = jnp.zeros((8, 384), F32)
    window = lax.div(wide * me, 128)
    for k in range(4):
        rows = r.dmod_flat[k, pl.ds(window, 3), :]
        for m in range(3):
            r.mod_pad[k : k + 1, 128 * m : 128 * m + 128] = rows[m : m + 1, :]
    o_dmod[...] = pltpu.roll(r.mod_pad[...], lax.rem(384 - lax.rem(wide * me, 128), 384), 1)[:, 0:256]
    small = jnp.sum(gain * gain) + jnp.sum(mask_row * mask_row)
    conds = [r.conds_all[k][0:1].astype(BF).astype(F32) for k in range(4)]
    for k in range(4):
        for m in range(k, 4):
            term = jnp.sum(mods[k] * mods[m]) * jnp.sum(conds[k] * conds[m])
            small += term if m == k else 2.0 * term
    got(S.sq, r.sq.at[0:31])
    total = r.sq[0]
    for k in range(1, ALL):
        total += r.sq[k]
    o_norm[...] = jnp.broadcast_to(jnp.sqrt(jnp.sum(total) + small), (8, 128))

    for at, like in drains:
        left(at, like)


def run_layer(*args):
    shapes = (
        ((ROWS, WIDTH), BF),
        ((ROWS, WIDTH), F32),
        ((8, 128), F32),
        ((24, 3 * WIDTH), F32),
        ((24, WIDTH), F32),
        ((24, 4 * WIDTH), F32),
        ((96, WIDTH), F32),
        ((8, 256), F32),
        ((16, 128), F32),
        ((16, 128), F32),
        ((8, 128), F32),
    )
    whole = pl.BlockSpec(memory_space=pltpu.VMEM)
    return pl.pallas_call(
        layer_kernel,
        out_shape=[jax.ShapeDtypeStruct(shape, kind) for shape, kind in shapes],
        in_specs=[pl.BlockSpec(memory_space=pl.ANY)] * len(args),
        out_specs=[whole] * len(shapes),
        scratch_shapes=[pltpu.VMEM(shape, kind) for shape, kind in SCRATCH.values()]
        + [pltpu.SMEM((3, 1), jnp.int32)]
        + [pltpu.SemaphoreType.DMA((SEM_COUNT,)), pltpu.SemaphoreType.DMA((SEM_COUNT,))],
        compiler_params=pltpu.CompilerParams(
            collective_id=0, has_side_effects=True, vmem_limit_bytes=60 * 1024 * 1024
        ),
    )(*args)


def finish_kernel(
    y, dx, norm, g_qkv, g_attn, g_in, g_out, dmod, g_vec, own_vec, conds, *rest
):
    (w_ada, w_qkv, w_attn, w_in, w_out), moments, outs = rest[:5], rest[5:17], rest[17:]
    outs[0][0] = y[...]
    outs[1][0] = dx[...]
    outs[2][0, 0] = norm[0, 0]
    clip = jnp.minimum(1.0, CLIP / (norm[0:1, 0:1] + 1e-06))
    columns = w_ada.shape[0]
    rounded = conds[...].astype(BF).astype(F32)
    turned_mod = dmod[...].T
    g_ada = turned_mod[0:columns, 0:1] * rounded[0:1, :]
    for k in range(1, 4):
        g_ada += turned_mod[0:columns, k : k + 1] * rounded[k : k + 1, :]
    narrow = moments[0].shape[1]
    grads = (
        g_vec[0:9, 0:narrow],
        g_ada,
        g_qkv[...],
        g_attn[...],
        g_in[...],
        g_out[...],
    )
    weights = (
        own_vec[0:9, 0:narrow],
        w_ada[...],
        w_qkv[...],
        w_attn[...],
        w_in[...],
        w_out[...],
    )
    for k in range(6):
        results = adam_step(
            weights[k],
            grads[k] * clip,
            moments[2 * k][...],
            moments[2 * k + 1][...],
            RATE if k else RATE_VECTORS,
            DECAY if k else 0.0,
        )
        for n in range(3):
            outs[3 + 3 * k + n][...] = results[n]


def run_finish(partial_results, weights, moments):
    shapes = [((1, ROWS, WIDTH), BF), ((1, ROWS, WIDTH), F32), ((1, 1), F32)]
    for moment in moments[::2]:
        shapes += [(moment.shape, F32)] * 3
    whole = pl.BlockSpec(memory_space=pltpu.VMEM)
    specs = [whole] * len(shapes)
    specs[2] = pl.BlockSpec(memory_space=pltpu.SMEM)
    args = (*partial_results, *weights, *moments)
    return pl.pallas_call(
        finish_kernel,
        out_shape=[jax.ShapeDtypeStruct(shape, kind) for shape, kind in shapes],
        in_specs=[whole] * len(args),
        out_specs=specs,
        compiler_params=pltpu.CompilerParams(vmem_limit_bytes=60 * 1024 * 1024),
    )(*args)


def slices(
    tokens_in,
    cotangent,
    timesteps,
    span_start,
    span_len,
    vectors,
    w_ada,
    w_qkv,
    w_attn,
    w_in,
    w_out,
    m_vec,
    v_vec,
    m_ada,
    v_ada,
    m_qkv,
    v_qkv,
    m_attn,
    v_attn,
    m_in,
    v_in,
    m_out,
    v_out,
):
    partial_results = run_layer(
        timesteps,
        span_start,
        span_len,
        tokens_in,
        cotangent,
        vectors,
        w_ada.T,
        w_qkv,
        w_attn,
        w_in,
        w_out,
    )
    moments = (
        m_vec,
        v_vec,
        m_ada.T,
        v_ada.T,
        m_qkv,
        v_qkv,
        m_attn,
        v_attn,
        m_in,
        v_in,
        m_out,
        v_out,
    )
    results = run_finish(partial_results, (w_ada.T, w_qkv, w_attn, w_in, w_out), moments)
    ada_results = [result.T for result in results[6:9]]
    return (*results[:2], results[2].reshape(()), *results[3:6], *ada_results, *results[9:])


def solution(mesh):
    in_specs = (
        P("dp", "seq", None),
        P("dp", "seq", None),
        P("dp"),
        P("dp"),
        P("dp"),
        P(),
        P(None, ("dp", "seq")),
        P(("dp", "seq"), None),
        P(("dp", "seq"), None),
        P(("dp", "seq"), None),
        P(("dp", "seq"), None),
        P(None, ("dp", "seq")),
        P(None, ("dp", "seq")),
        P(None, ("dp", "seq")),
        P(None, ("dp", "seq")),
        P(("dp", "seq"), None),
        P(("dp", "seq"), None),
        P(("dp", "seq"), None),
        P(("dp", "seq"), None),
        P(("dp", "seq"), None),
        P(("dp", "seq"), None),
        P(("dp", "seq"), None),
        P(("dp", "seq"), None),
    )
    out_specs = (
        P("dp", "seq", None),
        P("dp", "seq", None),
        P(),
        P(None, ("dp", "seq")),
        P(None, ("dp", "seq")),
        P(None, ("dp", "seq")),
        P(None, ("dp", "seq")),
        P(None, ("dp", "seq")),
        P(None, ("dp", "seq")),
        P(("dp", "seq"), None),
        P(("dp", "seq"), None),
        P(("dp", "seq"), None),
        P(("dp", "seq"), None),
        P(("dp", "seq"), None),
        P(("dp", "seq"), None),
        P(("dp", "seq"), None),
        P(("dp", "seq"), None),
        P(("dp", "seq"), None),
        P(("dp", "seq"), None),
        P(("dp", "seq"), None),
        P(("dp", "seq"), None),
    )
    sizes = dict(mesh.shape)
    local = slices if (sizes["dp"], sizes["seq"]) == (4, 8) else plain
    return jax.shard_map(local, mesh=mesh, in_specs=in_specs, out_specs=out_specs, check_vma=False)
```

```python
from functools import partial
import math
from types import SimpleNamespace

import jax
import jax.numpy as jnp
from jax import lax
from jax.experimental import pallas as pl
from jax.experimental.pallas import tpu as pltpu
from jax.sharding import PartitionSpec as P

HD = 64
COND = 128
STEP = 10


BETA_ONE = 0.9
BETA_TWO = 0.999
ADAM_EPS = 1e-08
RATE = 0.1
RATE_VECTORS = 0.3
DECAY = 0.01
CLIP = 1.0
NORM_EPS = 1e-05


def cond_input(timesteps):
    half_cond = COND // 2
    freqs = jnp.exp(jnp.arange(half_cond, dtype=jnp.float32) * (-math.log(10000.0) / half_cond))
    angles = timesteps.astype(jnp.float32)[:, None] * freqs[None, :]
    return jax.nn.silu(jnp.concatenate([jnp.cos(angles), jnp.sin(angles)], axis=1))


def rotary_tables(positions):
    half_head = HD // 2
    inverse = jnp.exp(jnp.arange(half_head, dtype=jnp.float32) * (-math.log(10000.0) / half_head))
    angles = positions.astype(jnp.float32)[:, None] * inverse[None, :]
    return (jnp.cos(angles), jnp.sin(angles))


def rotate(values, cosines, sines):
    half_head = values.shape[-1] // 2
    first = values[..., :half_head]
    second = values[..., half_head:]
    cos_b = cosines[:, None, :]
    sin_b = sines[:, None, :]
    return jnp.concatenate(
        [first * cos_b - second * sin_b, second * cos_b + first * sin_b], axis=-1
    )


def rotate_back(grads, cosines, sines):
    half_head = grads.shape[-1] // 2
    first = grads[..., :half_head]
    second = grads[..., half_head:]
    cos_b = cosines[:, None, :]
    sin_b = sines[:, None, :]
    return jnp.concatenate(
        [first * cos_b + second * sin_b, second * cos_b - first * sin_b], axis=-1
    )


def normalize(values):
    centre = jnp.mean(values, axis=-1, keepdims=True)
    centred = values - centre
    inverse = lax.rsqrt(jnp.mean(centred * centred, axis=-1, keepdims=True) + NORM_EPS)
    return (centred * inverse, inverse)


def norm_back(normed, inverse, grad):
    return inverse * (
        grad
        - jnp.mean(grad, axis=-1, keepdims=True)
        - normed * jnp.mean(grad * normed, axis=-1, keepdims=True)
    )


def split_kv(block, width):
    seqs, block_rows = (block.shape[0], block.shape[1])
    keys = block[..., :width].reshape(seqs, block_rows, width // HD, HD)
    values = block[..., width:].reshape(seqs, block_rows, width // HD, HD)
    return (keys, values)


def attend_piece(carry, piece, queries, width, factor):
    piece_rows = piece.shape[1]
    size = math.gcd(piece_rows, 512)

    def attend_one_block(index, state):
        running, denom, accum = state
        block = lax.dynamic_slice_in_dim(piece, index * size, size, 1)
        keys, values = split_kv(block, width)
        scores = (
            jnp.einsum("sqhd,skhd->shqk", queries, keys, preferred_element_type=jnp.float32)
            * factor
        )
        highest = jnp.maximum(running, jnp.max(scores, axis=-1))
        shrink = jnp.exp(running - highest)
        weights = jnp.exp(scores - highest[..., None])
        denom = denom * shrink + jnp.sum(weights, axis=-1)
        accum = accum * shrink[..., None] + jnp.einsum(
            "shqk,skhd->shqd",
            weights.astype(jnp.bfloat16),
            values,
            preferred_element_type=jnp.float32,
        )
        return (highest, denom, accum)

    return lax.fori_loop(0, piece_rows // size, attend_one_block, carry)


def block_grads(block, queries, grad_out, logsum, delta, width, factor):
    keys, values = split_kv(block, width)
    scores = (
        jnp.einsum("sqhd,skhd->shqk", queries, keys, preferred_element_type=jnp.float32) * factor
    )
    probs = jnp.exp(scores - logsum[..., None])
    dprobs = jnp.einsum("sqhd,skhd->shqk", grad_out, values, preferred_element_type=jnp.float32)
    dscores = (probs * (dprobs - delta[..., None])).astype(jnp.bfloat16)
    return (keys, probs, dscores)


def query_grads(kv_all, queries, grad_out, logsum, delta, width, factor):
    total_rows = kv_all.shape[1]
    size = math.gcd(total_rows, 512)

    def query_one_block(index, accum):
        block = lax.dynamic_slice_in_dim(kv_all, index * size, size, 1)
        keys, probs, dscores = block_grads(block, queries, grad_out, logsum, delta, width, factor)
        return accum + factor * jnp.einsum(
            "shqk,skhd->sqhd", dscores, keys, preferred_element_type=jnp.float32
        )

    return lax.fori_loop(
        0, total_rows // size, query_one_block, jnp.zeros(queries.shape, jnp.float32)
    )


def key_grads(kv_all, queries, grad_out, logsum, delta, width, factor, count):
    size = math.gcd(count, 512)
    seqs = queries.shape[0]

    def key_one_block(index, accum):
        block = lax.dynamic_slice_in_dim(kv_all, index * size, size, 1)
        keys, probs, dscores = block_grads(block, queries, grad_out, logsum, delta, width, factor)
        grad_vals = jnp.einsum(
            "shqk,sqhd->skhd",
            probs.astype(jnp.bfloat16),
            grad_out,
            preferred_element_type=jnp.float32,
        )
        grad_keys = factor * jnp.einsum(
            "shqk,sqhd->skhd", dscores, queries, preferred_element_type=jnp.float32
        )
        joined = jnp.concatenate(
            [grad_keys.reshape(seqs, size, width), grad_vals.reshape(seqs, size, width)], axis=-1
        )
        return lax.dynamic_update_slice_in_dim(
            accum, jnp.transpose(joined, (1, 0, 2)), index * size, 0
        )

    initial = jnp.zeros((count, seqs, 2 * width), jnp.float32)
    return lax.fori_loop(0, count // size, key_one_block, initial)


def adam_step(weight, grad, first, second, rate, decay_rate):
    new_first = BETA_ONE * first + (1.0 - BETA_ONE) * grad
    new_second = BETA_TWO * second + (1.0 - BETA_TWO) * grad * grad
    fixed_first = new_first / (1.0 - BETA_ONE**STEP)
    fixed_second = new_second / (1.0 - BETA_TWO**STEP)
    new_weight = weight - rate * (
        fixed_first / (jnp.sqrt(fixed_second) + ADAM_EPS) + decay_rate * weight
    )
    return (new_first, new_second, new_weight)


def mod_back(grad_hidden, ln_values, normed, scale_part, gain):
    grad_shift = jnp.sum(grad_hidden, axis=1)
    grad_scale = jnp.sum(grad_hidden * ln_values, axis=1)
    grad_ln = grad_hidden * (1.0 + scale_part)
    grad_gain = jnp.sum(grad_ln * normed, axis=(0, 1))
    return (grad_shift, grad_scale, grad_gain, grad_ln * gain)


def plain(
    tokens_in,
    cotangent,
    timesteps,
    span_start,
    span_len,
    vectors,
    w_ada,
    w_qkv,
    w_attn,
    w_in,
    w_out,
    m_vec,
    v_vec,
    m_ada,
    v_ada,
    m_qkv,
    v_qkv,
    m_attn,
    v_attn,
    m_in,
    v_in,
    m_out,
    v_out,
):
    seqs, group, width = tokens_in.shape
    heads = width // HD
    factor = HD ** (-0.5)
    flat_rows = seqs * group
    full_ada, full_qkv, full_attn, full_in, full_out = (
        lax.all_gather(w_ada.astype(jnp.bfloat16), ("dp", "seq"), axis=1, tiled=True),
        lax.all_gather(w_qkv.astype(jnp.bfloat16), ("dp", "seq"), axis=0, tiled=True),
        lax.all_gather(w_attn.astype(jnp.bfloat16), ("dp", "seq"), axis=0, tiled=True),
        lax.all_gather(w_in.astype(jnp.bfloat16), ("dp", "seq"), axis=0, tiled=True),
        lax.all_gather(w_out.astype(jnp.bfloat16), ("dp", "seq"), axis=0, tiled=True),
    )
    positions = lax.axis_index("seq") * group + jnp.arange(group, dtype=jnp.int32)
    masked = (positions[None, :] >= span_start[:, None]) & (
        positions[None, :] < (span_start + span_len)[:, None]
    )
    cond_bf = cond_input(timesteps).astype(jnp.bfloat16)
    modulation = jnp.dot(cond_bf, full_ada, preferred_element_type=jnp.float32) + vectors[
        2:8
    ].reshape(1, 6 * width)
    pieces = [modulation[:, which * width : (which + 1) * width][:, None, :] for which in range(6)]
    shift_one, scale_one, gate_one, shift_two, scale_two, gate_two = pieces
    start_tokens = jnp.where(
        masked[..., None], vectors[8][None, None, :], tokens_in.astype(jnp.float32)
    )
    normed_one, inv_one = normalize(start_tokens)
    ln_one = normed_one * vectors[0]
    hidden_one = (
        (ln_one * (1.0 + scale_one) + shift_one).astype(jnp.bfloat16).reshape(flat_rows, width)
    )
    projected = jnp.dot(hidden_one, full_qkv, preferred_element_type=jnp.float32).reshape(
        seqs, group, 3 * width
    )
    cosines, sines = rotary_tables(positions)
    queries = rotate(projected[..., :width].reshape(seqs, group, heads, HD), cosines, sines).astype(
        jnp.bfloat16
    )
    keys_here = rotate(
        projected[..., width : 2 * width].reshape(seqs, group, heads, HD), cosines, sines
    ).astype(jnp.bfloat16)
    values_here = projected[..., 2 * width :].astype(jnp.bfloat16)
    kv_local = jnp.concatenate([keys_here.reshape(seqs, group, width), values_here], axis=-1)
    initial = (
        jnp.full((seqs, heads, group), -1e30, jnp.float32),
        jnp.zeros((seqs, heads, group), jnp.float32),
        jnp.zeros((seqs, heads, group, HD), jnp.float32),
    )
    running, denom, accum = attend_piece(
        initial, lax.all_gather(kv_local, "seq", axis=1, tiled=True), queries, width, factor
    )
    attn_heads = accum / denom[..., None]
    logsum = running + jnp.log(denom)
    attn_rows = jnp.transpose(attn_heads, (0, 2, 1, 3)).reshape(flat_rows, width)
    attn_bf = attn_rows.astype(jnp.bfloat16)
    branch_one = jnp.dot(attn_bf, full_attn, preferred_element_type=jnp.float32).reshape(
        seqs, group, width
    )
    mid_tokens = start_tokens + gate_one * branch_one
    normed_two, inv_two = normalize(mid_tokens)
    ln_two = normed_two * vectors[1]
    hidden_two = (
        (ln_two * (1.0 + scale_two) + shift_two).astype(jnp.bfloat16).reshape(flat_rows, width)
    )
    pre_act = jnp.dot(hidden_two, full_in, preferred_element_type=jnp.float32)
    activ, gelu_back = jax.vjp(partial(jax.nn.gelu, approximate=True), pre_act)
    activ_bf = activ.astype(jnp.bfloat16)
    branch_two = jnp.dot(activ_bf, full_out, preferred_element_type=jnp.float32).reshape(
        seqs, group, width
    )
    block_out = (mid_tokens + gate_two * branch_two).astype(jnp.bfloat16)
    grad_y = cotangent.astype(jnp.float32)
    grad_gate_two = jnp.sum(grad_y * branch_two, axis=1)
    grad_branch_two = (grad_y * gate_two).astype(jnp.bfloat16).reshape(flat_rows, width)
    grad_w_out = jnp.dot(activ_bf.T, grad_branch_two, preferred_element_type=jnp.float32)
    grad_activ = jnp.dot(grad_branch_two, full_out.T, preferred_element_type=jnp.float32)
    grad_pre = gelu_back(grad_activ)[0].astype(jnp.bfloat16)
    grad_w_in = jnp.dot(hidden_two.T, grad_pre, preferred_element_type=jnp.float32)
    grad_hidden_two = jnp.dot(grad_pre, full_in.T, preferred_element_type=jnp.float32).reshape(
        seqs, group, width
    )
    grad_shift_two, grad_scale_two, grad_gain_two, grad_normed_two = mod_back(
        grad_hidden_two, ln_two, normed_two, scale_two, vectors[1]
    )
    grad_mid = grad_y + norm_back(normed_two, inv_two, grad_normed_two)
    grad_gate_one = jnp.sum(grad_mid * branch_one, axis=1)
    grad_branch_one = (grad_mid * gate_one).astype(jnp.bfloat16).reshape(flat_rows, width)
    grad_w_attn = jnp.dot(attn_bf.T, grad_branch_one, preferred_element_type=jnp.float32)
    grad_attn_bf = (
        jnp.dot(grad_branch_one, full_attn.T, preferred_element_type=jnp.float32)
        .astype(jnp.bfloat16)
        .reshape(seqs, group, heads, HD)
    )
    delta = jnp.einsum("sqhd,shqd->shq", grad_attn_bf.astype(jnp.float32), attn_heads)
    kv_all = lax.all_gather(kv_local, "seq", axis=1, tiled=True)
    grad_queries = query_grads(kv_all, queries, grad_attn_bf, logsum, delta, width, factor)
    grad_kv = jnp.transpose(
        lax.psum_scatter(
            key_grads(
                kv_all,
                queries,
                grad_attn_bf,
                logsum,
                delta,
                width,
                factor,
                group * lax.axis_size("seq"),
            ).astype(jnp.bfloat16),
            "seq",
            scatter_dimension=0,
            tiled=True,
        ).astype(jnp.float32),
        (1, 0, 2),
    )
    grad_keys = grad_kv[..., :width].reshape(seqs, group, heads, HD)
    grad_qkv = jnp.concatenate(
        [
            rotate_back(grad_queries, cosines, sines).reshape(seqs, group, width),
            rotate_back(grad_keys, cosines, sines).reshape(seqs, group, width),
            grad_kv[..., width:],
        ],
        axis=-1,
    )
    grad_qkv = grad_qkv.astype(jnp.bfloat16).reshape(flat_rows, 3 * width)
    grad_w_qkv = jnp.dot(hidden_one.T, grad_qkv, preferred_element_type=jnp.float32)
    grad_hidden_one = jnp.dot(grad_qkv, full_qkv.T, preferred_element_type=jnp.float32).reshape(
        seqs, group, width
    )
    grad_shift_one, grad_scale_one, grad_gain_one, grad_normed_one = mod_back(
        grad_hidden_one, ln_one, normed_one, scale_one, vectors[0]
    )
    grad_start = grad_mid + norm_back(normed_one, inv_one, grad_normed_one)
    grad_mask_row = jnp.sum(jnp.where(masked[..., None], grad_start, 0.0), axis=(0, 1))
    grad_input = jnp.where(masked[..., None], 0.0, grad_start)
    grad_mod = jnp.concatenate(
        [
            grad_shift_one,
            grad_scale_one,
            grad_gate_one,
            grad_shift_two,
            grad_scale_two,
            grad_gate_two,
        ],
        axis=1,
    )
    grad_w_ada = jnp.dot(cond_bf.astype(jnp.float32).T, grad_mod, precision=lax.Precision.HIGHEST)
    grad_vectors = jnp.concatenate(
        [
            grad_gain_one[None, :],
            grad_gain_two[None, :],
            jnp.sum(grad_mod, axis=0).reshape(6, width),
            grad_mask_row[None, :],
        ],
        axis=0,
    )
    red_ada, red_qkv, red_attn, red_in, red_out, red_vec = (
        lax.psum_scatter(grad_w_ada, ("dp", "seq"), scatter_dimension=1, tiled=True),
        lax.psum_scatter(grad_w_qkv, ("dp", "seq"), scatter_dimension=0, tiled=True),
        lax.psum_scatter(grad_w_attn, ("dp", "seq"), scatter_dimension=0, tiled=True),
        lax.psum_scatter(grad_w_in, ("dp", "seq"), scatter_dimension=0, tiled=True),
        lax.psum_scatter(grad_w_out, ("dp", "seq"), scatter_dimension=0, tiled=True),
        lax.psum_scatter(grad_vectors, ("dp", "seq"), scatter_dimension=1, tiled=True),
    )
    local_squares = jnp.float32(0.0)
    for reduced in (red_vec, red_ada, red_qkv, red_attn, red_in, red_out):
        local_squares = local_squares + jnp.sum(reduced * reduced)
    grad_norm = jnp.sqrt(lax.psum(local_squares, ("dp", "seq")))
    clip_factor = jnp.minimum(1.0, CLIP / (grad_norm + 1e-06))
    columns = red_vec.shape[1]
    own_vectors = lax.dynamic_slice_in_dim(
        vectors, lax.axis_index(("dp", "seq")) * columns, columns, 1
    )
    vec_out = adam_step(own_vectors, red_vec * clip_factor, m_vec, v_vec, RATE_VECTORS, 0.0)
    ada_out = adam_step(w_ada, red_ada * clip_factor, m_ada, v_ada, RATE, DECAY)
    qkv_out = adam_step(w_qkv, red_qkv * clip_factor, m_qkv, v_qkv, RATE, DECAY)
    attn_out = adam_step(w_attn, red_attn * clip_factor, m_attn, v_attn, RATE, DECAY)
    in_out = adam_step(w_in, red_in * clip_factor, m_in, v_in, RATE, DECAY)
    out_out = adam_step(w_out, red_out * clip_factor, m_out, v_out, RATE, DECAY)
    return (
        block_out,
        grad_input,
        grad_norm,
        vec_out[0],
        vec_out[1],
        vec_out[2],
        ada_out[0],
        ada_out[1],
        ada_out[2],
        qkv_out[0],
        qkv_out[1],
        qkv_out[2],
        attn_out[0],
        attn_out[1],
        attn_out[2],
        in_out[0],
        in_out[1],
        in_out[2],
        out_out[0],
        out_out[1],
        out_out[2],
    )


F32, BF = jnp.float32, jnp.bfloat16
MESH = pl.DeviceIdType.MESH
DP, LINE, SEQ, CHIPS, ALL = 4, 4, 8, 16, 32
ROWS, WIDTH, PACK = 128, 768, 640
HALF = WIDTH // 2
HALVES = ((0, 0), (0, 1), (0, 2), (2, 2), (1, 0), (1, 1), (1, 2), None, (2, 0), (2, 1))

def numbered(**counts):
    at = {}
    for name, count in counts.items():
        at[name] = sum(counts[other] for other in at)
    return SimpleNamespace(**at), sum(counts.values())


S, SEM_COUNT = numbered(
    load=11,
    cond=1,
    mix_qkv=1,
    mix_in=1,
    mix_attn=1,
    mod=1,
    w_qkv=1,
    w_attn=1,
    plane_in=1,
    w_in=4,
    w_out=4,
    group_qkv=4,
    group_attn=4,
    fw_qkv=1,
    fw_attn=1,
    fw_in=1,
    fw_out=1,
    tok=4,
    h2=4,
    dm=4,
    xf=4,
    o=1,
    mm=1,
    dh2=1,
    do=1,
    gp=1,
    dh1=5,
    pair_out=1,
    pair_in=1,
    pair_attn=1,
    pair_qkv=1,
    plane_attn=1,
    plane_qkv=1,
    line_out=5,
    line_in=5,
    slice_in=1,
    line_attn=1,
    line_qkv=1,
    last_in=1,
    last_attn=1,
    last_qkv=1,
    early=1,
    early2=1,
    late=1,
    late2=1,
    sq=1,
)

SCRATCH = dict(
    i_tok=((1, 128, 768), BF),
    i_cot=((1, 128, 768), BF),
    i_vec=((9, 768), F32),
    i_wada=((144, 128), F32),
    i_wqkv=((24, 2304), F32),
    i_wattn=((24, 768), F32),
    i_win=((24, 3072), F32),
    i_wout=((96, 768), F32),
    wide_qkv=((48, 3072), F32),
    wide_in=((48, 3072), F32),
    wide_attn=((48, 768), F32),
    s_qkv=((48, 3072), BF),
    s_in=((48, 3072), BF),
    s_attn=((48, 768), BF),
    w_qkv=((768, 768), BF),
    w_in=((4, 4, 48, 768), BF),
    w_attn=((768, 768), BF),
    w_out=((4, 2, 96, 768), BF),
    conds_all=((4, 8, 128), F32),
    mod_send=((4, 4, 128), F32),
    mod_got=((32, 4, 128), F32),
    mod_flat=((40, 128), F32),
    mod_pad=((8, 384), F32),
    turn=((2, 4, 128, 128), F32),
    dmod_flat=((4, 40, 128), F32),
    mod=((8, 768), F32),
    x0=((128, 768), F32),
    n1=((128, 768), F32),
    inv1=((128, 128), F32),
    x1=((128, 768), F32),
    n2=((128, 768), F32),
    inv2=((128, 128), F32),
    a=((128, 768), F32),
    dx1=((128, 768), F32),
    toks=((4, 128, 768), BF),
    h1=((4, 128, 768), BF),
    h2=((4, 128, 768), BF),
    dm=((4, 128, 768), BF),
    gb=((4, 128, 768), BF),
    du=((4, 128, 768), BF),
    xb=((2, 4, 128, 640), BF),
    pt=((3, 1024, 512), BF),
    vt=((2, 128, 1024), BF),
    kt=((2, 128, 1024), BF),
    back=((4, 128, 768), F32),
    ot=((2, 128, 512), F32),
    os=((4, 192, 128), BF),
    ob=((4, 192, 128), BF),
    o2=((4, 128, 128), BF),
    mms=((4, 128, 768), BF),
    mmr=((4, 128, 768), BF),
    dhs=((4, 128, 768), BF),
    dhr=((4, 128, 768), BF),
    das=((128, 768), BF),
    dos=((4, 192, 128), BF),
    dob=((4, 192, 128), BF),
    dst=((3, 1024, 512), BF),
    ga=((512, 640), F32),
    gps=((512, 512), BF),
    gpr=((512, 512), BF),
    dqkv=((4, 128, 768), BF),
    d1s=((4, 128, 768), BF),
    d1r=((4, 128, 768), BF),
    g_out=((4, 2, 96, 768), BF),
    g_in=((2, 4, 4, 48, 384), BF),
    g_attn=((2, 768, 384), BF),
    g_qkv=((2, 768, 384), BF),
    p_out=((4, 96, 768), BF),
    p_in=((4, 4, 48, 384), BF),
    p_attn=((768, 384), BF),
    p_qkv=((768, 384), BF),
    q_attn=((4, 192, 384), BF),
    q_qkv=((4, 192, 384), BF),
    m_attn=((192, 384), BF),
    m_qkv=((192, 384), BF),
    r_out=((4, 96, 768), BF),
    r_in=((4, 4, 48, 384), BF),
    via_in=((4, 48, 384), BF),
    via_out=((96, 768), BF),
    via_dh1=((128, 768), BF),
    m_in=((4, 48, 384), BF),
    u_in=((4, 48, 384), BF),
    r_attn=((4, 48, 384), BF),
    r_qkv=((4, 48, 384), BF),
    t_in=((4, 48, 384), F32),
    t_attn=((1, 48, 384), F32),
    t_qkv=((4, 48, 384), F32),
    f_in=((4, 2, 24, 384), F32),
    f_attn=((1, 2, 24, 384), F32),
    f_qkv=((4, 2, 24, 384), F32),
    early=((8, 768), F32),
    early_got=((8, 8, 768), F32),
    early_all=((4, 8, 768), F32),
    late=((4, 768), F32),
    late_got=((8, 4, 768), F32),
    late_all=((4, 4, 768), F32),
    sq=((32, 1, 128), F32),
)


def dot(left, right):
    return jnp.dot(left, right, preferred_element_type=F32)


def dot_nt(left, right):
    return lax.dot_general(left, right, (((1,), (1,)), ((), ())), preferred_element_type=F32)


def dot_tn(left, right):
    return lax.dot_general(left, right, (((0,), (0,)), ((), ())), preferred_element_type=F32)


def loop(count, body, start=0):
    def step(index, carry):
        body(index)
        return carry

    lax.fori_loop(start, count, step, 0)


def layer_kernel(
    i_time,
    i_start,
    i_len,
    h_tok,
    h_cot,
    h_vec,
    h_wada,
    h_wqkv,
    h_wattn,
    h_win,
    h_wout,
    o_y,
    o_dx,
    o_norm,
    o_gqkv,
    o_gattn,
    o_gin,
    o_gout,
    o_dmod,
    o_gvec,
    o_vec,
    o_conds,
    *scratch,
):
    r = SimpleNamespace(**dict(zip(SCRATCH, scratch)), when=scratch[-3])
    send_sems, recv_sems = scratch[-2:]
    i_tok, i_cot, i_vec, i_wada = r.i_tok, r.i_cot, r.i_vec, r.i_wada
    i_wqkv, i_wattn, i_win, i_wout = r.i_wqkv, r.i_wattn, r.i_win, r.i_wout
    b, s = lax.axis_index("dp"), lax.axis_index("seq")
    z, c = lax.div(s, 2), lax.rem(s, 2)
    mate = s + 1 - 2 * c
    chip = b * LINE + z
    me = b * SEQ + s
    drains = []

    def push(src, dst, at, to_b, to_s, out=None):
        pltpu.make_async_remote_copy(
            src_ref=src,
            dst_ref=dst,
            send_sem=send_sems.at[at if out is None else out],
            recv_sem=recv_sems.at[at],
            device_id=(to_b, to_s),
            device_id_type=MESH,
        ).start()

    def keep(src, dst, at):
        pltpu.make_async_copy(src, dst, recv_sems.at[at]).start()

    def got(at, like):
        pltpu.make_async_copy(like, like, recv_sems.at[at]).wait()

    def left(at, like):
        pltpu.make_async_copy(like, like, send_sems.at[at]).wait()

    def sent(at, like):
        drains.append((at, like))

    near = (b, b + 1 - 2 * lax.rem(b, 2), b + 2 - 4 * lax.div(b, 2), 3 - b)

    def toward(k):
        if k == 3:
            return 3, near[3]
        slot = 1 + c if k == 1 else 2 - c
        return slot, (1 - c) * near[k] + c * near[3 - k]

    def peers(body):
        for k in (1, 2, 3):
            body(*toward(k))

    def stack(body):
        for k in (1, 2, 3):
            body(lax.rem(z + k + 2 * c * (2 - k), LINE))

    def line_gather(block, at, near=True, rest=True):
        inner = 1 + lax.rem(z, 2)
        if near:
            push(block(z), block(z), at + z, b, 2 * inner + c, at)

        def one(to):
            relayed = ((z == 1) & (to == 3)) | ((z == 2) & (to == 0))

            @pl.when(jnp.logical_not(relayed | (to == inner)))
            def _():
                push(block(z), block(z), at + z, b, 2 * to + c, at)

        if rest:
            stack(one)

    def line_relay(block, at):
        for middle, source, to in ((2, 1, 3), (1, 2, 0)):

            @pl.when(z == middle)
            def _():
                got(at + source, block(source))
                push(block(source), block(source), at + source, b, 2 * to + c, at)

    def line_got(block, at, k):
        here = (k == z) | ((z == 2) & (k == 1)) | ((z == 1) & (k == 2))

        @pl.when(jnp.logical_not(here))
        def _():
            got(at + k, block(0))

    far = lax.div(z, 2)

    def line_order(j):
        return lax.rem(z + (2, 3 - 2 * far, 1 + 2 * far, 0)[j], LINE)

    def line_add(j, rows, dst, via, at):
        to = line_order(j)
        outer_chip = (z == 0) | (z == 3)

        def direct():
            push(rows(to), dst.at[z], at + z, b, 2 * to + c, at)

        if j == 0:

            @pl.when(outer_chip)
            def _():
                push(rows(to), via, at + 4, b, 2 * (1 + far) + c, at)

            @pl.when(jnp.logical_not(outer_chip))
            def _():
                direct()

        elif j < 3:
            direct()
        else:
            keep(rows(z), dst.at[z], at + z)

    def line_via(via, at, add):
        @pl.when((z == 1) | (z == 2))
        def _():
            got(at + 4, via)
            add()

    def line_done(dst, at):
        for k in range(4):
            missing = ((z == 1) & (k == 3)) | ((z == 2) & (k == 0))

            @pl.when(jnp.logical_not(missing))
            def _():
                got(at + k, dst.at[k])

    def line_clear(dst):
        for middle, k in ((1, 3), (2, 0)):

            @pl.when(z == middle)
            def _():
                dst[k] = jnp.zeros(dst.shape[1:], BF)

    lane = lax.broadcasted_iota(jnp.int32, (1, 128), 1)
    low = lane < 64
    own24 = pl.ds(pl.multiple_of(24 * c, 8), 24)
    mate24 = pl.ds(pl.multiple_of(24 * (1 - c), 8), 24)
    part = pl.ds(pl.multiple_of(HALF * c, 128), HALF)
    chip_rows = pl.ds(pl.multiple_of(48 * chip, 16), 48)
    group_rows = pl.ds(pl.multiple_of(192 * b, 16), 192)

    barrier = pltpu.get_barrier_semaphore()

    def greet(k):
        other = lax.rem(me + k, ALL)
        pl.semaphore_signal(
            barrier, inc=1, device_id=(lax.div(other, SEQ), lax.rem(other, SEQ)), device_id_type=MESH
        )

    loads = (
        (i_time, r.when.at[0]),
        (i_start, r.when.at[1]),
        (i_len, r.when.at[2]),
        (h_wqkv, i_wqkv),
        (h_win, i_win),
        (h_wattn, i_wattn),
        (h_wout, i_wout),
        (h_tok, i_tok),
        (h_vec, i_vec),
        (h_wada, i_wada),
        (h_cot, i_cot),
    )
    for k, (src, dst) in enumerate(loads):
        pltpu.make_async_copy(src, dst, recv_sems.at[S.load + k]).start()
    loop(ALL, greet, 1)
    for k, (src, dst) in enumerate(loads):
        pltpu.make_async_copy(src, dst, recv_sems.at[S.load + k]).wait()

    def natural(kind, p, head):
        return kind * WIDTH + 192 * p + 64 * head

    def half_at(ref, column, high):
        tile = ref[:, column // 128 * 128 : column // 128 * 128 + 128]
        return tile if (column % 128 == 64) == high else pltpu.roll(tile, 64, 1)

    for p in range(4):
        for tile in range(5):
            pair = []
            for high in (0, 1):
                which = HALVES[2 * tile + high]
                pair.append(
                    jnp.zeros((24, 128), F32)
                    if which is None
                    else half_at(i_wqkv, natural(which[0], p, which[1]), bool(high))
                )
            r.wide_qkv[own24, 768 * p + 128 * tile : 768 * p + 128 * tile + 128] = jnp.where(
                low, pair[0], pair[1]
            )
        r.wide_qkv[own24, 768 * p + 640 : 768 * p + 768] = jnp.zeros((24, 128), F32)
    r.wide_in[own24, :] = i_win[...]
    r.wide_attn[own24, :] = i_wattn[...]
    r.w_out[z, c] = i_wout[...].astype(BF)
    r.toks[z] = i_tok[0]
    line_clear(r.r_out)
    line_clear(r.r_in)
    line_clear(r.d1r)
    lanes8 = lax.broadcasted_iota(jnp.int32, (8, 128), 1)
    half_cond = COND // 2
    speed = jnp.exp((lanes8 % half_cond).astype(F32) * (-math.log(10000.0) / half_cond))
    angle = r.when[0, 0].astype(F32) * speed
    wave = jnp.where(lanes8 < half_cond, jnp.cos(angle), jnp.sin(angle))
    r.conds_all[b] = wave * (1.0 / (1.0 + jnp.exp(-wave)))
    pl.semaphore_wait(barrier, ALL - 1)

    def token_block(k):
        return r.toks.at[k]

    def in_block(k):
        return r.w_in.at[:, k, :, part]

    def out_block(k):
        return r.w_out.at[k, c]

    peers(lambda k, to: push(r.conds_all.at[b], r.conds_all.at[b], S.cond, to, s))
    sent(S.cond, r.conds_all.at[0:3])
    push(r.wide_qkv.at[own24], r.wide_qkv.at[own24], S.mix_qkv, b, mate)
    sent(S.mix_qkv, r.wide_qkv.at[0:24])
    push(r.wide_attn.at[own24], r.wide_attn.at[own24], S.mix_attn, b, mate)
    sent(S.mix_attn, r.wide_attn.at[0:24])
    push(r.wide_in.at[own24], r.wide_in.at[own24], S.mix_in, b, mate)
    sent(S.mix_in, r.wide_in.at[0:24])

    got(S.cond, r.conds_all.at[0:3])
    row8 = lax.broadcasted_iota(jnp.int32, (8, 128), 0)
    cond4 = jnp.zeros((8, 128), F32)
    for k in range(4):
        cond4 = jnp.where(row8 == k, r.conds_all[k], cond4)
    o_conds[...] = cond4
    wide = i_wada.shape[0]
    r.mod_pad[...] = jnp.zeros((8, 384), F32)
    r.mod_pad[:, 0:wide] = dot_nt(cond4.astype(BF), i_wada[...].astype(BF))
    columns = pltpu.roll(r.mod_pad[...], lax.rem(wide * me, 128), 1)
    for k in range(4):
        for t in range(3):
            r.mod_send[k, t : t + 1, :] = columns[k : k + 1, 128 * t : 128 * t + 128]
        r.mod_send[k, 3:4, :] = jnp.zeros((1, 128), F32)

    def send_mod(k):
        other = lax.rem(me + k, ALL)
        ob = lax.div(other, SEQ)
        push(r.mod_send.at[ob], r.mod_got.at[me], S.mod, ob, lax.rem(other, SEQ))

    loop(ALL, send_mod, 1)
    sent(S.mod, r.mod_got.at[0:31])
    keep(r.mod_send.at[b], r.mod_got.at[me], S.mod)

    def block(src, first):
        return src.at[:, pl.ds(pl.multiple_of(first, 128), HALF)]

    def along_line(src, dst, at, step):
        stack(
            lambda to: push(
                block(src, step * to + HALF * c), dst.at[chip_rows, part], at, b, 2 * to + c
            )
        )
        keep(block(src, step * z + HALF * c), dst.at[chip_rows, part], at)
        sent(at, dst.at[0:144, 0:HALF])

    def over_plane(dst, first, at):
        got(first, dst.at[0:192, 0:HALF])
        rows = dst.at[group_rows, part]
        peers(lambda k, to: push(rows, rows, at + k, to, s))
        for k in (1, 2, 3):
            sent(at + k, dst.at[0:192, 0:HALF])

    def share(dst, at, onward):
        for k in range(4):
            rows = dst.at[pl.ds(pl.multiple_of(192 * near[k], 16), 192), part]
            if k:
                got(at + k, rows)
            push(rows, rows, onward, b, mate)
        sent(onward, dst.at[:, 0:HALF])

    def line_share(block, at, onward):
        for k in range(4):
            line_got(block, at, k)
            push(block(k), block(k), onward, b, mate)

    got(S.mix_qkv, r.wide_qkv.at[0:24])
    r.s_qkv[...] = r.wide_qkv[...].astype(BF)
    along_line(r.s_qkv, r.w_qkv, S.w_qkv, WIDTH)
    line_gather(token_block, S.tok, rest=False)
    sent(S.tok, r.toks.at[0:3])
    got(S.mix_attn, r.wide_attn.at[0:24])
    r.s_attn[...] = r.wide_attn[...].astype(BF)
    over_plane(r.w_qkv, S.w_qkv, S.group_qkv)
    line_gather(token_block, S.tok, near=False)
    along_line(r.s_attn, r.w_attn, S.w_attn, 0)
    line_gather(out_block, S.w_out)
    sent(S.w_out, r.w_out.at[0:3, 0])
    got(S.mix_in, r.wide_in.at[0:24])
    r.s_in[...] = r.wide_in[...].astype(BF)
    peers(
        lambda k, to: push(
            block(r.s_in, WIDTH * to + HALF * c), r.w_in.at[b, z, :, part], S.plane_in, to, s
        )
    )
    keep(block(r.s_in, WIDTH * b + HALF * c), r.w_in.at[b, z, :, part], S.plane_in)
    sent(S.plane_in, r.w_in.at[0:3, 0, :, 0:HALF])

    def start_tokens(tokens, k):
        place = (2 * k + c) * ROWS + lax.broadcasted_iota(jnp.int32, (ROWS, 1), 0)
        hidden = (place >= r.when[1, 0]) & (place < r.when[1, 0] + r.when[2, 0])
        return jnp.where(hidden, i_vec[8:9, :], tokens.astype(F32)), hidden

    x0, _ = start_tokens(i_tok[0], z)
    r.x0[...] = x0
    n1, inv1 = normalize(x0)
    r.n1[...] = n1
    r.inv1[...] = jnp.broadcast_to(inv1, (ROWS, 128))

    got(S.mod, r.mod_got)
    r.mod_flat[...] = jnp.zeros((40, 128), F32)
    for k in range(ALL):
        first = 9 * k // 8
        r.mod_flat[first : first + 3, :] += r.mod_got[k, 0:3, :]
    for k in range(6):
        row = jnp.concatenate(
            [r.mod_flat[6 * k + t : 6 * k + t + 1, :] for t in range(6)], axis=1
        )
        r.mod[k : k + 1, :] = row + i_vec[2 + k : 3 + k, :]

    def mod(k):
        return r.mod[k : k + 1, :]

    def vec(k):
        return i_vec[k : k + 1, :]

    r.h1[z] = (r.n1[...] * vec(0) * (1.0 + mod(1)) + mod(0)).astype(BF)
    r.dm[0] = (i_cot[0].astype(F32) * mod(5)).astype(BF)
    peers(lambda k, to: push(r.dm.at[0], r.dm.at[k], S.dm + k, to, s))
    for k in (1, 2, 3):
        sent(S.dm + k, r.dm.at[0])

    lanes = lax.broadcasted_iota(jnp.int32, (ROWS, 128), 1)
    first_half = lanes % HD < HD // 2
    speed = jnp.exp((lanes % (HD // 2)).astype(F32) * (-math.log(10000.0) / (HD // 2)))
    row = lax.broadcasted_iota(jnp.int32, (ROWS, 128), 0)

    def table(k):
        angle = ((2 * k + c) * ROWS + row).astype(F32) * speed
        r.turn[0, k] = jnp.cos(angle)
        sine = jnp.sin(angle)
        r.turn[1, k] = jnp.where(first_half, -sine, sine)

    loop(LINE, table)

    line_relay(token_block, S.tok)

    share(r.w_qkv, S.group_qkv, S.fw_qkv)
    got(S.fw_qkv, r.w_qkv.at[:, 0:HALF])

    def turned(tile, sign, k):
        other = jnp.where(first_half, pltpu.roll(tile, 96, 1), pltpu.roll(tile, 32, 1))
        return tile * r.turn[0, k] + sign * (other * r.turn[1, k])

    def project(j):
        k = lax.rem(z + j, LINE)

        @pl.when(j > 0)
        def _():
            line_got(token_block, S.tok, k)
            other, _ = start_tokens(r.toks[k], k)
            other, _ = normalize(other)
            r.h1[k] = (other * vec(0) * (1.0 + mod(1)) + mod(0)).astype(BF)

        x = dot(r.h1[k], r.w_qkv[:, 0:PACK])
        tiles = [x[:, 128 * t : 128 * t + 128] for t in range(5)]
        tiles[0] = turned(tiles[0], 1.0, k) * 0.125
        tiles[1] = jnp.where(low, turned(tiles[1], 1.0, k) * 0.125, tiles[1])
        tiles[2] = turned(tiles[2], 1.0, k)
        tiles[3] = turned(tiles[3], 1.0, k)
        for t in range(5):
            r.xb[0, k, :, 128 * t : 128 * t + 128] = tiles[t].astype(BF)
        push(r.xb.at[0, k], r.xb.at[1, k], S.xf + k, b, mate)

    loop(4, project)
    over_plane(r.w_attn, S.w_attn, S.group_attn)
    for k in range(4):
        sent(S.xf + k, r.xb.at[0, 0])

    for k in range(4):
        got(S.xf + k, r.xb.at[0, 0])

    def tile_of(t):
        return r.xb[:, :, :, 128 * t : 128 * t + 128].reshape(1024, 128)

    heads = ((0, 2, 4, True, True), (0, 2, 4, False, False), (1, 3, 1, True, False))

    def queries(head, first, size):
        q_tile, _, _, q_low, _ = heads[head]
        q = r.xb[0, first : first + size, :, 128 * q_tile : 128 * q_tile + 128]
        return jnp.where(low if q_low else ~low, q.reshape(size * 128, 128), jnp.zeros((), BF))

    r.vt[0] = tile_of(4).T
    r.vt[1] = tile_of(1).T
    for half in range(2):
        at = slice(256 * half, 256 * half + 256)
        for head in range(3):
            scores = dot_nt(tile_of(heads[head][1]), queries(head, 2 * half, 2))
            weights = jnp.exp(scores - jnp.max(scores, axis=0, keepdims=True))
            weights = weights * (1.0 / jnp.sum(weights, axis=0, keepdims=True))
            weights = weights.astype(BF)
            r.pt[head, :, at] = weights
            out = dot(r.vt[head // 2], weights)
            if head == 0:
                r.ot[0, 0:64, at] = out[0:64]
            elif head == 1:
                r.ot[0, 64:128, at] = out[64:128]
            else:
                r.ot[1, 0:64, at] = out[64:128]
                r.ot[1, 64:128, at] = jnp.zeros((64, 256), F32)
        for k in (2 * half, 2 * half + 1):
            across = slice(128 * k, 128 * k + 128)
            r.os[k, 0:128, :] = r.ot[0, :, across].T.astype(BF)
            third = r.ot[1, 0:64, across]
            third = jnp.concatenate([third, pltpu.roll(third, 64, 1)], axis=0)
            r.os[k, 128:192, :] = third.T[0:64].astype(BF)
        for to in (2 * half, 2 * half + 1):

            @pl.when(z == to)
            def _():
                keep(r.os.at[to], r.ob.at[z], S.o)

            @pl.when(z != to)
            def _():
                push(r.os.at[to], r.ob.at[z], S.o, b, 2 * to + c)

        if half == 0:
            line_relay(out_block, S.w_out)

    sent(S.o, r.os.at[0:3])
    got(S.plane_in, r.w_in.at[:, 0, :, 0:HALF])
    line_gather(in_block, S.w_in)
    sent(S.w_in, r.w_in.at[0:3, :, :, 0:HALF])
    for k in range(2):
        r.kt[k] = tile_of(2 + k).T
    share(r.w_attn, S.group_attn, S.fw_attn)
    got(S.fw_attn, r.w_attn.at[:, 0:HALF])
    got(S.o, r.ob)
    a = jnp.zeros((ROWS, WIDTH), F32)
    for p in range(4):
        third = r.ob[p, 128:192, :].astype(F32)
        third = jnp.concatenate([third, pltpu.roll(third, 64, 1)], axis=0)
        r.o2[p] = jnp.where(low, third, 0.0).astype(BF)
        a += dot(r.ob[p, 0:128, :], r.w_attn[192 * p : 192 * p + 128, :])
        a += dot(r.o2[p, :, 0:64], r.w_attn[192 * p + 128 : 192 * p + 192, :])
    r.a[...] = a
    x1 = r.x0[...] + mod(2) * a
    r.x1[...] = x1
    n2, inv2 = normalize(x1)
    r.n2[...] = n2
    r.inv2[...] = jnp.broadcast_to(inv2, (ROWS, 128))
    r.h2[0] = (n2 * vec(1) * (1.0 + mod(4)) + mod(3)).astype(BF)
    peers(lambda k, to: push(r.h2.at[0], r.h2.at[k], S.h2 + k, to, s))
    for k in (1, 2, 3):
        sent(S.h2 + k, r.h2.at[0])
    line_relay(in_block, S.w_in)
    line_share(out_block, S.w_out, S.fw_out)
    sent(S.fw_out, r.w_out.at[:, 0])
    got(S.fw_out, r.w_out.at[:, 0])

    def feed_back(k):
        @pl.when(k > 0)
        def _():
            got(S.dm + k, r.dm.at[0])

        r.back[k] = dot_nt(r.dm[k], r.w_out[...].reshape(WIDTH, WIDTH))

    loop(4, feed_back)
    line_share(in_block, S.w_in, S.fw_in)
    sent(S.fw_in, r.w_in.at[:, :, :, 0:HALF])
    got(S.fw_in, r.w_in.at[:, :, :, 0:HALF])

    def feed(first, count):
        at = slice(first, first + count)
        size = count * ROWS
        u = dot(r.h2[at].reshape(size, WIDTH), r.w_in[...].reshape(WIDTH, WIDTH))
        slope = 0.7978845608028654
        cube = 0.044715
        t = jnp.tanh(slope * (u + cube * u * u * u))
        r.gb[at] = (0.5 * u * (1.0 + t)).astype(BF).reshape(count, ROWS, WIDTH)
        bend = 0.5 * (1.0 + t) + 0.5 * u * (1.0 - t * t) * (slope * (1.0 + 3.0 * cube * u * u))
        du = (r.back[at].reshape(size, WIDTH) * bend).astype(BF)
        r.du[at] = du.reshape(count, ROWS, WIDTH)
        r.dhs[at] = dot_nt(du, r.w_in[...].reshape(WIDTH, WIDTH)).astype(BF).reshape(count, ROWS, WIDTH)

    feed(0, 1)
    for first, count in ((1, 2), (3, 1)):
        for k in range(first, first + count):
            got(S.h2 + k, r.h2.at[0])
        feed(first, count)
        for k in range(first, first + count):
            slot, to = toward(k)
            push(r.dhs.at[slot], r.dhr.at[slot], S.dh2, to, s)
    sent(S.dh2, r.dhs.at[0:3])
    def gather(own, others):
        total = own[0].astype(F32)
        for k in (1, 2, 3):
            total += others[k].astype(F32)
        return total

    for k in range(2):
        rows = slice(384 * k, 384 * k + 384)
        result = dot_tn(r.gb[:, :, rows].reshape(512, 384), r.dm[...].reshape(512, 768))
        r.g_out[2 * k : 2 * k + 2] = result.astype(BF).reshape(2, 2, 96, 768)
    push(r.g_out.at[:, 1 - c], r.p_out, S.pair_out, b, mate)
    sent(S.pair_out, r.p_out)

    def outer(left, right, dst):
        for k in range(2):
            rows = slice(384 * k, 384 * k + 384)
            result = dot_tn(
                left[:, :, rows].reshape(512, 384), right[...].reshape(512, 768)
            ).astype(BF)
            dst[0, rows, :] = result[:, 0:HALF]
            dst[1, rows, :] = result[:, HALF:WIDTH]

    def to_mate(grad, dst, at):
        push(grad.at[1 - c], dst, at, b, mate)
        sent(at, dst)

    def pair_sum(grad, pair, at):
        got(at, pair)
        grad[c] = (grad[c].astype(F32) + pair[...].astype(F32)).astype(BF)

    def plane_sum(grad, dst, at):
        def rows(to):
            return grad.at[c, pl.ds(pl.multiple_of(192 * to, 16), 192)]

        peers(lambda k, to: push(rows(to), dst.at[k], at, to, s))
        keep(rows(b), dst.at[0], at)
        sent(at, dst.at[0:3])

    def line_sum(src, total, dst, first, at):
        got(first, src)
        total[...] = (
            (src[0].astype(F32) + src[1].astype(F32)) + (src[2].astype(F32) + src[3].astype(F32))
        ).astype(BF)

        def rows(to):
            return total.at[pl.ds(pl.multiple_of(48 * to, 16), 48)]

        stack(lambda to: push(rows(to), dst.at[z], at, b, 2 * to + c))
        keep(rows(z), dst.at[z], at)
        sent(at, dst.at[0:3])

    def trade(total, final, at):
        push(total.at[:, mate24], final.at[:, c], at, b, mate)
        sent(at, final.at[:, 0])
        final[:, c] = total[:, own24, :]

    for k in range(2):
        rows = slice(384 * k, 384 * k + 384)
        result = dot_tn(r.h2[:, :, rows].reshape(512, 384), r.du[...].reshape(512, 768)).astype(BF)
        for h in range(2):
            r.g_in[h, 2 * k : 2 * k + 2] = result[:, 384 * h : 384 * h + 384].reshape(2, 4, 48, 384)
    to_mate(r.g_in, r.p_in, S.pair_in)

    got(S.pair_out, r.p_out)
    for k in range(4):
        r.g_out[k, c] = (r.g_out[k, c].astype(F32) + r.p_out[k].astype(F32)).astype(BF)

    def out_rows(k):
        return r.g_out.at[k, c]

    for j in (0, 1):
        line_add(j, out_rows, r.r_out, r.via_out, S.line_out)

    def add_out():
        k = line_order(2)
        r.g_out[k, c] = (r.g_out[k, c].astype(F32) + r.via_out[...].astype(F32)).astype(BF)

    got(S.dh2, r.dhr.at[0:3])
    dh = gather(r.dhs, r.dhr)
    n2 = r.n2[...]
    inv2 = r.inv2[:, 0:1]
    r.early[...] = jnp.zeros((8, 768), F32)
    r.early[2:3, :] = jnp.sum(dh, axis=0, keepdims=True)
    both = jnp.sum(dh * n2, axis=0, keepdims=True)
    r.early[3:4, :] = both * vec(1)
    r.early[0:1, :] = both * (1.0 + mod(4))
    grad = dh * ((1.0 + mod(4)) * vec(1))
    dx1 = i_cot[0].astype(F32) + norm_back(n2, inv2, grad)
    r.dx1[...] = dx1
    r.early[1:2, :] = jnp.sum(dx1 * r.a[...], axis=0, keepdims=True)
    r.das[...] = (dx1 * mod(2)).astype(BF)
    for p in range(4):
        first = 192 * p
        r.dos[p, 0:128, :] = dot_nt(r.das[...], r.w_attn[first : first + 128, :]).astype(BF)
        tail = dot_nt(r.das[...], r.w_attn[first + 128 : first + 192, :])
        tail = jnp.concatenate([tail, jnp.zeros((ROWS, 64), F32)], axis=1)
        r.dos[p, 128:192, :] = jnp.where(low, tail[0:64], pltpu.roll(tail[64:128], 64, 1)).astype(
            BF
        )

    stack(lambda to: push(r.dos.at[to], r.dob.at[z], S.do, b, 2 * to + c))
    keep(r.dos.at[z], r.dob.at[z], S.do)
    sent(S.do, r.dos.at[0:3])
    for t in range(3):
        at = slice(256 * t, 256 * t + 256)
        mm = dot(r.gb[...].reshape(512, WIDTH), r.w_out[:, :, :, at].reshape(WIDTH, 256))
        r.mms[:, :, at] = mm.astype(BF).reshape(4, ROWS, 256)
    peers(lambda k, to: push(r.mms.at[k], r.mmr.at[k], S.mm, to, s))
    sent(S.mm, r.mms.at[0:3])

    for p in range(4):
        for rows, left_side in (
            (slice(192 * p, 192 * p + 128), r.ob[p, 0:128, :]),
            (slice(192 * p + 128, 192 * p + 192), r.o2[p]),
        ):
            result = dot_tn(left_side, r.das[...])[0 : rows.stop - rows.start].astype(BF)
            r.g_attn[0, rows, :] = result[:, 0:HALF]
            r.g_attn[1, rows, :] = result[:, HALF:WIDTH]
    to_mate(r.g_attn, r.p_attn, S.pair_attn)

    def over_line(src, dst, name):
        def one(k):
            push(src, dst.at[s], name, b, lax.rem(s + k, SEQ))

        loop(SEQ, one, 1)
        keep(src, dst.at[s], name)
        sent(name, dst.at[0:7])

    def over_group(got_ref, dst, name):
        total = got_ref[0]
        for k in range(1, SEQ):
            total += got_ref[k]
        dst[b] = total
        peers(lambda k, to: push(dst.at[b], dst.at[b], name, to, s))
        sent(name, dst.at[0:3])


    pair_sum(r.g_in, r.p_in, S.pair_in)

    line_via(r.via_out, S.line_out, add_out)
    for j in (2, 3):
        line_add(j, out_rows, r.r_out, r.via_out, S.line_out)
    sent(S.line_out, r.r_out.at[0:3])

    def in_rows(k):
        return r.g_in.at[c, :, k]

    for j in (0, 1):
        line_add(j, in_rows, r.r_in, r.via_in, S.line_in)

    def add_in():
        k = line_order(2)
        r.g_in[c, :, k] = (r.g_in[c, :, k].astype(F32) + r.via_in[...].astype(F32)).astype(BF)

    pair_sum(r.g_attn, r.p_attn, S.pair_attn)
    plane_sum(r.g_attn, r.q_attn, S.plane_attn)

    got(S.do, r.dob)
    dot0 = r.dob[:, 0:128, :].reshape(512, 128)
    third = r.dob[:, 128:192, :].astype(F32).reshape(256, 128)
    other_rows = jnp.where(low, pltpu.roll(third, 64, 1), 0.0).reshape(4, 64, 128)
    third = jnp.where(low, third, 0.0).reshape(4, 64, 128)
    dot1 = jnp.concatenate([third, other_rows], axis=1).reshape(512, 128)
    zero = jnp.zeros((), BF)
    moved = pltpu.roll(dot1, 64, 1).astype(BF)
    grads = (jnp.where(low, dot0, zero), jnp.where(low, zero, dot0), moved)
    product = dot0.astype(F32).T * r.ot[0]
    deltas = (
        jnp.sum(product[0:64], axis=0, keepdims=True),
        jnp.sum(product[64:128], axis=0, keepdims=True),
        jnp.sum(dot1.T * r.ot[1], axis=0, keepdims=True),
    )
    for head in range(3):
        values = tile_of(heads[head][2])
        for half in range(2):
            at = slice(256 * half, 256 * half + 256)
            dp = dot_nt(values, grads[head][at])
            r.dst[head, :, at] = (
                r.pt[head, :, at].astype(F32) * (dp - deltas[head][:, at])
            ).astype(BF)

    def key_grads(rows):
        dk = [dot(r.dst[head, rows, :], queries(head, 0, 4)) for head in range(3)]
        dv = [dot(r.pt[head, rows, :], grads[head]) for head in range(3)]
        return (dv[2], dk[0] + dk[1], dk[2], dv[0] + dv[1])

    line_via(r.via_in, S.line_in, add_in)
    for j in (2, 3):
        line_add(j, in_rows, r.r_in, r.via_in, S.line_in)
    sent(S.line_in, r.r_in.at[0:3])
    for t, tile in enumerate(key_grads(slice(512, 1024))):
        r.gps[:, 128 * t : 128 * t + 128] = tile.astype(BF)
    push(r.gps, r.gpr, S.gp, b, mate)
    sent(S.gp, r.gps)
    for t, tile in enumerate(key_grads(slice(0, 512))):
        r.ga[:, 128 * t + 128 : 128 * t + 256] = tile
    for half in range(2):
        at = slice(256 * half, 256 * half + 256)
        turned_q = [dot(r.kt[head // 2], r.dst[head, :, at]) for head in range(3)]
        top = jnp.concatenate([turned_q[0][0:64], turned_q[1][64:128]], axis=0)
        r.ga[at, 0:128] = top.T * 0.125
        r.ga[at, 128:256] += turned_q[2].T * 0.125
    got(S.mm, r.mmr.at[0:3])
    mm = gather(r.mms, r.mmr)
    o_y[...] = (r.x1[...] + mod(5) * mm).astype(BF)
    r.early[4:5, :] = jnp.sum(i_cot[0].astype(F32) * mm, axis=0, keepdims=True)
    over_line(r.early, r.early_got, S.early)
    got(S.gp, r.gpr)

    def dh1_rows(k):
        return r.d1s.at[k]

    def back_turn(k):
        rows = pl.ds(pl.multiple_of(128 * k, 128), 128)
        tiles = [r.ga[rows, 0:128]] + [
            r.ga[rows, 128 * t : 128 * t + 128]
            + r.gpr[rows, 128 * t - 128 : 128 * t].astype(F32)
            for t in range(1, 5)
        ]
        tiles[0] = turned(tiles[0], -1.0, k)
        tiles[1] = jnp.where(low, turned(tiles[1], -1.0, k), tiles[1])
        tiles[2] = turned(tiles[2], -1.0, k)
        tiles[3] = turned(tiles[3], -1.0, k)
        for t in range(5):
            r.dqkv[k, :, 128 * t : 128 * t + 128] = tiles[t].astype(BF)
        r.dqkv[k, :, PACK:WIDTH] = jnp.zeros((128, 128), BF)

    loop(4, back_turn)

    def unproject(j):
        k = line_order(j)
        partial_sum = dot_nt(r.dqkv[k, :, 0:PACK], r.w_qkv[:, 0:PACK])
        r.d1s[k] = partial_sum.astype(BF)
        if j == 2:

            def add():
                r.d1s[k] = (partial_sum + r.via_dh1[...].astype(F32)).astype(BF)

            line_via(r.via_dh1, S.dh1, add)
        line_add(j, dh1_rows, r.d1r, r.via_dh1, S.dh1)

    unproject(0)
    outer(r.h1, r.dqkv, r.g_qkv)
    to_mate(r.g_qkv, r.p_qkv, S.pair_qkv)
    unproject(1)
    pair_sum(r.g_qkv, r.p_qkv, S.pair_qkv)
    plane_sum(r.g_qkv, r.q_qkv, S.plane_qkv)
    unproject(2)
    unproject(3)
    sent(S.dh1, r.d1s.at[0:3])
    line_sum(r.q_attn, r.m_attn, r.r_attn, S.plane_attn, S.line_attn)
    got(S.early, r.early_got)
    over_group(r.early_got, r.early_all, S.early2)

    line_done(r.r_in, S.line_in)
    r.m_in[...] = (
        (r.r_in[0].astype(F32) + r.r_in[1].astype(F32))
        + (r.r_in[2].astype(F32) + r.r_in[3].astype(F32))
    ).astype(BF)
    peers(lambda k, to: push(r.m_in.at[to], r.u_in.at[b], S.slice_in, to, s))
    keep(r.m_in.at[b], r.u_in.at[b], S.slice_in)
    sent(S.slice_in, r.u_in.at[0:3])
    line_sum(r.q_qkv, r.m_qkv, r.r_qkv, S.plane_qkv, S.line_qkv)

    line_done(r.d1r, S.dh1)
    dh = (r.d1r[0].astype(F32) + r.d1r[1].astype(F32)) + (
        r.d1r[2].astype(F32) + r.d1r[3].astype(F32)
    )
    n1 = r.n1[...]
    both = jnp.sum(dh * n1, axis=0, keepdims=True)
    r.late[0:1, :] = both * (1.0 + mod(1))
    r.late[1:2, :] = jnp.sum(dh, axis=0, keepdims=True)
    r.late[2:3, :] = both * vec(0)
    grad = dh * ((1.0 + mod(1)) * vec(0))
    dx0 = r.dx1[...] + norm_back(n1, r.inv1[:, 0:1], grad)
    _, hidden = start_tokens(i_tok[0], z)
    o_dx[...] = jnp.where(hidden, 0.0, dx0)
    r.late[3:4, :] = jnp.sum(jnp.where(hidden, dx0, 0.0), axis=0, keepdims=True)
    over_line(r.late, r.late_got, S.late)

    line_done(r.r_out, S.line_out)
    total = (r.r_out[0].astype(F32) + r.r_out[1].astype(F32)) + (
        r.r_out[2].astype(F32) + r.r_out[3].astype(F32)
    )
    o_gout[...] = total
    squares = total * total
    squares = jnp.sum(squares[:, 0:128] + squares[:, 128:256] + squares[:, 256:384]
                      + squares[:, 384:512] + squares[:, 512:640] + squares[:, 640:768],
                      axis=0, keepdims=True)

    def fold(value):
        total = value[:, 0:128] * value[:, 0:128]
        for t in range(1, value.shape[1] // 128):
            total += value[:, 128 * t : 128 * t + 128] * value[:, 128 * t : 128 * t + 128]
        return jnp.sum(total, axis=0, keepdims=True)

    got(S.slice_in, r.u_in)
    r.t_in[...] = r.u_in[...].astype(F32)
    for p in range(4):
        squares += fold(r.t_in[p])
    trade(r.t_in, r.f_in, S.last_in)
    got(S.line_attn, r.r_attn)
    r.t_attn[0] = (r.r_attn[0].astype(F32) + r.r_attn[1].astype(F32)) + (
        r.r_attn[2].astype(F32) + r.r_attn[3].astype(F32)
    )
    squares += fold(r.t_attn[0])
    trade(r.t_attn, r.f_attn, S.last_attn)
    got(S.line_qkv, r.r_qkv)
    r.t_qkv[...] = r.r_qkv[...].astype(F32)
    trade(r.t_qkv, r.f_qkv, S.last_qkv)
    for p in range(4):
        squares += fold(r.t_qkv[p])
    r.sq[me] = squares

    def send_sq(k):
        other = lax.rem(me + k, ALL)
        push(r.sq.at[me], r.sq.at[me], S.sq, lax.div(other, SEQ), lax.rem(other, SEQ))

    loop(ALL, send_sq, 1)
    sent(S.sq, r.sq.at[0:31])
    got(S.late, r.late_got)
    over_group(r.late_got, r.late_all, S.late2)
    got(S.last_in, r.f_in.at[:, 0])
    got(S.last_attn, r.f_attn.at[:, 0])
    for h in range(2):
        for p in range(4):
            value = r.f_in[p, h]
            o_gin[:, 768 * p + 384 * h : 768 * p + 384 * h + 384] = value
        value = r.f_attn[0, h]
        o_gattn[:, 384 * h : 384 * h + 384] = value
    got(S.last_qkv, r.f_qkv.at[:, 0])
    where = {which: index for index, which in enumerate(HALVES) if which is not None}

    def packed_half(chunk, high):
        kind, rest = chunk // 12, chunk % 12
        index = where[(kind, rest % 3)]
        t = index // 2
        tile = r.f_qkv[rest // 3, t // 3, :, t % 3 * 128 : t % 3 * 128 + 128]
        return tile if index % 2 == high else pltpu.roll(tile, 64, 1)

    for t in range(18):
        o_gqkv[:, 128 * t : 128 * t + 128] = jnp.where(
            low, packed_half(2 * t, 0), packed_half(2 * t + 1, 1)
        )
    got(S.early2, r.early_all.at[0:3])
    got(S.late2, r.late_all.at[0:3])
    mods = []
    for k in range(4):
        early, late = r.early_all[k], r.late_all[k]
        rows = jnp.concatenate([late[1:3], early[1:5], jnp.zeros((2, 768), F32)], axis=0)
        for n in range(6):
            for m in range(6):
                r.dmod_flat[k, 6 * n + m : 6 * n + m + 1, :] = rows[
                    n : n + 1, 128 * m : 128 * m + 128
                ]
        mods.append(rows)
    gain = jnp.concatenate(
        [
            sum(r.late_all[k][0:1] for k in range(4)),
            sum(r.early_all[k][0:1] for k in range(4)),
            (mods[0] + mods[1] + mods[2] + mods[3])[0:6],
        ],
        axis=0,
    )
    mask_row = sum(r.late_all[k][3:4] for k in range(4))
    gains = jnp.concatenate([gain, mask_row, jnp.zeros((7, 768), F32)], axis=0)
    masters = jnp.concatenate([i_vec[...], jnp.zeros((7, 768), F32)], axis=0)
    own = lax.rem(WIDTH - 24 * me, WIDTH)
    o_gvec[...] = pltpu.roll(gains, own, 1)[:, 0:128]
    o_vec[...] = pltpu.roll(masters, own, 1)[:, 0:128]
    r.mod_pad[...] = jnp.zeros((8, 384), F32)
    window = lax.div(wide * me, 128)
    for k in range(4):
        rows = r.dmod_flat[k, pl.ds(window, 3), :]
        for m in range(3):
            r.mod_pad[k : k + 1, 128 * m : 128 * m + 128] = rows[m : m + 1, :]
    o_dmod[...] = pltpu.roll(r.mod_pad[...], lax.rem(384 - lax.rem(wide * me, 128), 384), 1)[:, 0:256]
    small = jnp.sum(gain * gain) + jnp.sum(mask_row * mask_row)
    conds = [r.conds_all[k][0:1].astype(BF).astype(F32) for k in range(4)]
    for k in range(4):
        for m in range(k, 4):
            term = jnp.sum(mods[k] * mods[m]) * jnp.sum(conds[k] * conds[m])
            small += term if m == k else 2.0 * term
    got(S.sq, r.sq.at[0:31])
    total = r.sq[0]
    for k in range(1, ALL):
        total += r.sq[k]
    o_norm[...] = jnp.broadcast_to(jnp.sqrt(jnp.sum(total) + small), (8, 128))

    for at, like in drains:
        left(at, like)


def run_layer(*args):
    shapes = (
        ((ROWS, WIDTH), BF),
        ((ROWS, WIDTH), F32),
        ((8, 128), F32),
        ((24, 3 * WIDTH), F32),
        ((24, WIDTH), F32),
        ((24, 4 * WIDTH), F32),
        ((96, WIDTH), F32),
        ((8, 256), F32),
        ((16, 128), F32),
        ((16, 128), F32),
        ((8, 128), F32),
    )
    whole = pl.BlockSpec(memory_space=pltpu.VMEM)
    return pl.pallas_call(
        layer_kernel,
        out_shape=[jax.ShapeDtypeStruct(shape, kind) for shape, kind in shapes],
        in_specs=[pl.BlockSpec(memory_space=pl.ANY)] * len(args),
        out_specs=[whole] * len(shapes),
        scratch_shapes=[pltpu.VMEM(shape, kind) for shape, kind in SCRATCH.values()]
        + [pltpu.SMEM((3, 1), jnp.int32)]
        + [pltpu.SemaphoreType.DMA((SEM_COUNT,)), pltpu.SemaphoreType.DMA((SEM_COUNT,))],
        compiler_params=pltpu.CompilerParams(
            collective_id=0, has_side_effects=True, vmem_limit_bytes=60 * 1024 * 1024
        ),
    )(*args)


def finish_kernel(
    y, dx, norm, g_qkv, g_attn, g_in, g_out, dmod, g_vec, own_vec, conds, *rest
):
    (w_ada, w_qkv, w_attn, w_in, w_out), moments, outs = rest[:5], rest[5:17], rest[17:]
    outs[0][0] = y[...]
    outs[1][0] = dx[...]
    outs[2][0, 0] = norm[0, 0]
    clip = jnp.minimum(1.0, CLIP / (norm[0:1, 0:1] + 1e-06))
    columns = w_ada.shape[0]
    rounded = conds[...].astype(BF).astype(F32)
    turned_mod = dmod[...].T
    g_ada = turned_mod[0:columns, 0:1] * rounded[0:1, :]
    for k in range(1, 4):
        g_ada += turned_mod[0:columns, k : k + 1] * rounded[k : k + 1, :]
    narrow = moments[0].shape[1]
    grads = (
        g_vec[0:9, 0:narrow],
        g_ada,
        g_qkv[...],
        g_attn[...],
        g_in[...],
        g_out[...],
    )
    weights = (
        own_vec[0:9, 0:narrow],
        w_ada[...],
        w_qkv[...],
        w_attn[...],
        w_in[...],
        w_out[...],
    )
    for k in range(6):
        results = adam_step(
            weights[k],
            grads[k] * clip,
            moments[2 * k][...],
            moments[2 * k + 1][...],
            RATE if k else RATE_VECTORS,
            DECAY if k else 0.0,
        )
        for n in range(3):
            outs[3 + 3 * k + n][...] = results[n]


def run_finish(partial_results, weights, moments):
    shapes = [((1, ROWS, WIDTH), BF), ((1, ROWS, WIDTH), F32), ((1, 1), F32)]
    for moment in moments[::2]:
        shapes += [(moment.shape, F32)] * 3
    whole = pl.BlockSpec(memory_space=pltpu.VMEM)
    specs = [whole] * len(shapes)
    specs[2] = pl.BlockSpec(memory_space=pltpu.SMEM)
    args = (*partial_results, *weights, *moments)
    return pl.pallas_call(
        finish_kernel,
        out_shape=[jax.ShapeDtypeStruct(shape, kind) for shape, kind in shapes],
        in_specs=[whole] * len(args),
        out_specs=specs,
        compiler_params=pltpu.CompilerParams(vmem_limit_bytes=60 * 1024 * 1024),
    )(*args)


def slices(
    tokens_in,
    cotangent,
    timesteps,
    span_start,
    span_len,
    vectors,
    w_ada,
    w_qkv,
    w_attn,
    w_in,
    w_out,
    m_vec,
    v_vec,
    m_ada,
    v_ada,
    m_qkv,
    v_qkv,
    m_attn,
    v_attn,
    m_in,
    v_in,
    m_out,
    v_out,
):
    partial_results = run_layer(
        timesteps,
        span_start,
        span_len,
        tokens_in,
        cotangent,
        vectors,
        w_ada.T,
        w_qkv,
        w_attn,
        w_in,
        w_out,
    )
    moments = (
        m_vec,
        v_vec,
        m_ada.T,
        v_ada.T,
        m_qkv,
        v_qkv,
        m_attn,
        v_attn,
        m_in,
        v_in,
        m_out,
        v_out,
    )
    results = run_finish(partial_results, (w_ada.T, w_qkv, w_attn, w_in, w_out), moments)
    ada_results = [result.T for result in results[6:9]]
    return (*results[:2], results[2].reshape(()), *results[3:6], *ada_results, *results[9:])


def solution(mesh):
    in_specs = (
        P("dp", "seq", None),
        P("dp", "seq", None),
        P("dp"),
        P("dp"),
        P("dp"),
        P(),
        P(None, ("dp", "seq")),
        P(("dp", "seq"), None),
        P(("dp", "seq"), None),
        P(("dp", "seq"), None),
        P(("dp", "seq"), None),
        P(None, ("dp", "seq")),
        P(None, ("dp", "seq")),
        P(None, ("dp", "seq")),
        P(None, ("dp", "seq")),
        P(("dp", "seq"), None),
        P(("dp", "seq"), None),
        P(("dp", "seq"), None),
        P(("dp", "seq"), None),
        P(("dp", "seq"), None),
        P(("dp", "seq"), None),
        P(("dp", "seq"), None),
        P(("dp", "seq"), None),
    )
    out_specs = (
        P("dp", "seq", None),
        P("dp", "seq", None),
        P(),
        P(None, ("dp", "seq")),
        P(None, ("dp", "seq")),
        P(None, ("dp", "seq")),
        P(None, ("dp", "seq")),
        P(None, ("dp", "seq")),
        P(None, ("dp", "seq")),
        P(("dp", "seq"), None),
        P(("dp", "seq"), None),
        P(("dp", "seq"), None),
        P(("dp", "seq"), None),
        P(("dp", "seq"), None),
        P(("dp", "seq"), None),
        P(("dp", "seq"), None),
        P(("dp", "seq"), None),
        P(("dp", "seq"), None),
        P(("dp", "seq"), None),
        P(("dp", "seq"), None),
        P(("dp", "seq"), None),
    )
    sizes = dict(mesh.shape)
    local = slices if (sizes["dp"], sizes["seq"]) == (4, 8) else plain
    return jax.shard_map(local, mesh=mesh, in_specs=in_specs, out_specs=out_specs, check_vma=False)
```

```python
from functools import partial
import math
from types import SimpleNamespace

import jax
import jax.numpy as jnp
from jax import lax
from jax.experimental import pallas as pl
from jax.experimental.pallas import tpu as pltpu
from jax.sharding import PartitionSpec as P

HD = 64
COND = 128
STEP = 10


BETA_ONE = 0.9
BETA_TWO = 0.999
ADAM_EPS = 1e-08
RATE = 0.1
RATE_VECTORS = 0.3
DECAY = 0.01
CLIP = 1.0
NORM_EPS = 1e-05


def cond_input(timesteps):
    half_cond = COND // 2
    freqs = jnp.exp(jnp.arange(half_cond, dtype=jnp.float32) * (-math.log(10000.0) / half_cond))
    angles = timesteps.astype(jnp.float32)[:, None] * freqs[None, :]
    return jax.nn.silu(jnp.concatenate([jnp.cos(angles), jnp.sin(angles)], axis=1))


def rotary_tables(positions):
    half_head = HD // 2
    inverse = jnp.exp(jnp.arange(half_head, dtype=jnp.float32) * (-math.log(10000.0) / half_head))
    angles = positions.astype(jnp.float32)[:, None] * inverse[None, :]
    return (jnp.cos(angles), jnp.sin(angles))


def rotate(values, cosines, sines):
    half_head = values.shape[-1] // 2
    first = values[..., :half_head]
    second = values[..., half_head:]
    cos_b = cosines[:, None, :]
    sin_b = sines[:, None, :]
    return jnp.concatenate(
        [first * cos_b - second * sin_b, second * cos_b + first * sin_b], axis=-1
    )


def rotate_back(grads, cosines, sines):
    half_head = grads.shape[-1] // 2
    first = grads[..., :half_head]
    second = grads[..., half_head:]
    cos_b = cosines[:, None, :]
    sin_b = sines[:, None, :]
    return jnp.concatenate(
        [first * cos_b + second * sin_b, second * cos_b - first * sin_b], axis=-1
    )


def normalize(values):
    centre = jnp.mean(values, axis=-1, keepdims=True)
    centred = values - centre
    inverse = lax.rsqrt(jnp.mean(centred * centred, axis=-1, keepdims=True) + NORM_EPS)
    return (centred * inverse, inverse)


def norm_back(normed, inverse, grad):
    return inverse * (
        grad
        - jnp.mean(grad, axis=-1, keepdims=True)
        - normed * jnp.mean(grad * normed, axis=-1, keepdims=True)
    )


def split_kv(block, width):
    seqs, block_rows = (block.shape[0], block.shape[1])
    keys = block[..., :width].reshape(seqs, block_rows, width // HD, HD)
    values = block[..., width:].reshape(seqs, block_rows, width // HD, HD)
    return (keys, values)


def attend_piece(carry, piece, queries, width, factor):
    piece_rows = piece.shape[1]
    size = math.gcd(piece_rows, 512)

    def attend_one_block(index, state):
        running, denom, accum = state
        block = lax.dynamic_slice_in_dim(piece, index * size, size, 1)
        keys, values = split_kv(block, width)
        scores = (
            jnp.einsum("sqhd,skhd->shqk", queries, keys, preferred_element_type=jnp.float32)
            * factor
        )
        highest = jnp.maximum(running, jnp.max(scores, axis=-1))
        shrink = jnp.exp(running - highest)
        weights = jnp.exp(scores - highest[..., None])
        denom = denom * shrink + jnp.sum(weights, axis=-1)
        accum = accum * shrink[..., None] + jnp.einsum(
            "shqk,skhd->shqd",
            weights.astype(jnp.bfloat16),
            values,
            preferred_element_type=jnp.float32,
        )
        return (highest, denom, accum)

    return lax.fori_loop(0, piece_rows // size, attend_one_block, carry)


def block_grads(block, queries, grad_out, logsum, delta, width, factor):
    keys, values = split_kv(block, width)
    scores = (
        jnp.einsum("sqhd,skhd->shqk", queries, keys, preferred_element_type=jnp.float32) * factor
    )
    probs = jnp.exp(scores - logsum[..., None])
    dprobs = jnp.einsum("sqhd,skhd->shqk", grad_out, values, preferred_element_type=jnp.float32)
    dscores = (probs * (dprobs - delta[..., None])).astype(jnp.bfloat16)
    return (keys, probs, dscores)


def query_grads(kv_all, queries, grad_out, logsum, delta, width, factor):
    total_rows = kv_all.shape[1]
    size = math.gcd(total_rows, 512)

    def query_one_block(index, accum):
        block = lax.dynamic_slice_in_dim(kv_all, index * size, size, 1)
        keys, probs, dscores = block_grads(block, queries, grad_out, logsum, delta, width, factor)
        return accum + factor * jnp.einsum(
            "shqk,skhd->sqhd", dscores, keys, preferred_element_type=jnp.float32
        )

    return lax.fori_loop(
        0, total_rows // size, query_one_block, jnp.zeros(queries.shape, jnp.float32)
    )


def key_grads(kv_all, queries, grad_out, logsum, delta, width, factor, count):
    size = math.gcd(count, 512)
    seqs = queries.shape[0]

    def key_one_block(index, accum):
        block = lax.dynamic_slice_in_dim(kv_all, index * size, size, 1)
        keys, probs, dscores = block_grads(block, queries, grad_out, logsum, delta, width, factor)
        grad_vals = jnp.einsum(
            "shqk,sqhd->skhd",
            probs.astype(jnp.bfloat16),
            grad_out,
            preferred_element_type=jnp.float32,
        )
        grad_keys = factor * jnp.einsum(
            "shqk,sqhd->skhd", dscores, queries, preferred_element_type=jnp.float32
        )
        joined = jnp.concatenate(
            [grad_keys.reshape(seqs, size, width), grad_vals.reshape(seqs, size, width)], axis=-1
        )
        return lax.dynamic_update_slice_in_dim(
            accum, jnp.transpose(joined, (1, 0, 2)), index * size, 0
        )

    initial = jnp.zeros((count, seqs, 2 * width), jnp.float32)
    return lax.fori_loop(0, count // size, key_one_block, initial)


def adam_step(weight, grad, first, second, rate, decay_rate):
    new_first = BETA_ONE * first + (1.0 - BETA_ONE) * grad
    new_second = BETA_TWO * second + (1.0 - BETA_TWO) * grad * grad
    fixed_first = new_first / (1.0 - BETA_ONE**STEP)
    fixed_second = new_second / (1.0 - BETA_TWO**STEP)
    new_weight = weight - rate * (
        fixed_first / (jnp.sqrt(fixed_second) + ADAM_EPS) + decay_rate * weight
    )
    return (new_first, new_second, new_weight)


def mod_back(grad_hidden, ln_values, normed, scale_part, gain):
    grad_shift = jnp.sum(grad_hidden, axis=1)
    grad_scale = jnp.sum(grad_hidden * ln_values, axis=1)
    grad_ln = grad_hidden * (1.0 + scale_part)
    grad_gain = jnp.sum(grad_ln * normed, axis=(0, 1))
    return (grad_shift, grad_scale, grad_gain, grad_ln * gain)


def plain(
    tokens_in,
    cotangent,
    timesteps,
    span_start,
    span_len,
    vectors,
    w_ada,
    w_qkv,
    w_attn,
    w_in,
    w_out,
    m_vec,
    v_vec,
    m_ada,
    v_ada,
    m_qkv,
    v_qkv,
    m_attn,
    v_attn,
    m_in,
    v_in,
    m_out,
    v_out,
):
    seqs, group, width = tokens_in.shape
    heads = width // HD
    factor = HD ** (-0.5)
    flat_rows = seqs * group
    full_ada, full_qkv, full_attn, full_in, full_out = (
        lax.all_gather(w_ada.astype(jnp.bfloat16), ("dp", "seq"), axis=1, tiled=True),
        lax.all_gather(w_qkv.astype(jnp.bfloat16), ("dp", "seq"), axis=0, tiled=True),
        lax.all_gather(w_attn.astype(jnp.bfloat16), ("dp", "seq"), axis=0, tiled=True),
        lax.all_gather(w_in.astype(jnp.bfloat16), ("dp", "seq"), axis=0, tiled=True),
        lax.all_gather(w_out.astype(jnp.bfloat16), ("dp", "seq"), axis=0, tiled=True),
    )
    positions = lax.axis_index("seq") * group + jnp.arange(group, dtype=jnp.int32)
    masked = (positions[None, :] >= span_start[:, None]) & (
        positions[None, :] < (span_start + span_len)[:, None]
    )
    cond_bf = cond_input(timesteps).astype(jnp.bfloat16)
    modulation = jnp.dot(cond_bf, full_ada, preferred_element_type=jnp.float32) + vectors[
        2:8
    ].reshape(1, 6 * width)
    pieces = [modulation[:, which * width : (which + 1) * width][:, None, :] for which in range(6)]
    shift_one, scale_one, gate_one, shift_two, scale_two, gate_two = pieces
    start_tokens = jnp.where(
        masked[..., None], vectors[8][None, None, :], tokens_in.astype(jnp.float32)
    )
    normed_one, inv_one = normalize(start_tokens)
    ln_one = normed_one * vectors[0]
    hidden_one = (
        (ln_one * (1.0 + scale_one) + shift_one).astype(jnp.bfloat16).reshape(flat_rows, width)
    )
    projected = jnp.dot(hidden_one, full_qkv, preferred_element_type=jnp.float32).reshape(
        seqs, group, 3 * width
    )
    cosines, sines = rotary_tables(positions)
    queries = rotate(projected[..., :width].reshape(seqs, group, heads, HD), cosines, sines).astype(
        jnp.bfloat16
    )
    keys_here = rotate(
        projected[..., width : 2 * width].reshape(seqs, group, heads, HD), cosines, sines
    ).astype(jnp.bfloat16)
    values_here = projected[..., 2 * width :].astype(jnp.bfloat16)
    kv_local = jnp.concatenate([keys_here.reshape(seqs, group, width), values_here], axis=-1)
    initial = (
        jnp.full((seqs, heads, group), -1e30, jnp.float32),
        jnp.zeros((seqs, heads, group), jnp.float32),
        jnp.zeros((seqs, heads, group, HD), jnp.float32),
    )
    running, denom, accum = attend_piece(
        initial, lax.all_gather(kv_local, "seq", axis=1, tiled=True), queries, width, factor
    )
    attn_heads = accum / denom[..., None]
    logsum = running + jnp.log(denom)
    attn_rows = jnp.transpose(attn_heads, (0, 2, 1, 3)).reshape(flat_rows, width)
    attn_bf = attn_rows.astype(jnp.bfloat16)
    branch_one = jnp.dot(attn_bf, full_attn, preferred_element_type=jnp.float32).reshape(
        seqs, group, width
    )
    mid_tokens = start_tokens + gate_one * branch_one
    normed_two, inv_two = normalize(mid_tokens)
    ln_two = normed_two * vectors[1]
    hidden_two = (
        (ln_two * (1.0 + scale_two) + shift_two).astype(jnp.bfloat16).reshape(flat_rows, width)
    )
    pre_act = jnp.dot(hidden_two, full_in, preferred_element_type=jnp.float32)
    activ, gelu_back = jax.vjp(partial(jax.nn.gelu, approximate=True), pre_act)
    activ_bf = activ.astype(jnp.bfloat16)
    branch_two = jnp.dot(activ_bf, full_out, preferred_element_type=jnp.float32).reshape(
        seqs, group, width
    )
    block_out = (mid_tokens + gate_two * branch_two).astype(jnp.bfloat16)
    grad_y = cotangent.astype(jnp.float32)
    grad_gate_two = jnp.sum(grad_y * branch_two, axis=1)
    grad_branch_two = (grad_y * gate_two).astype(jnp.bfloat16).reshape(flat_rows, width)
    grad_w_out = jnp.dot(activ_bf.T, grad_branch_two, preferred_element_type=jnp.float32)
    grad_activ = jnp.dot(grad_branch_two, full_out.T, preferred_element_type=jnp.float32)
    grad_pre = gelu_back(grad_activ)[0].astype(jnp.bfloat16)
    grad_w_in = jnp.dot(hidden_two.T, grad_pre, preferred_element_type=jnp.float32)
    grad_hidden_two = jnp.dot(grad_pre, full_in.T, preferred_element_type=jnp.float32).reshape(
        seqs, group, width
    )
    grad_shift_two, grad_scale_two, grad_gain_two, grad_normed_two = mod_back(
        grad_hidden_two, ln_two, normed_two, scale_two, vectors[1]
    )
    grad_mid = grad_y + norm_back(normed_two, inv_two, grad_normed_two)
    grad_gate_one = jnp.sum(grad_mid * branch_one, axis=1)
    grad_branch_one = (grad_mid * gate_one).astype(jnp.bfloat16).reshape(flat_rows, width)
    grad_w_attn = jnp.dot(attn_bf.T, grad_branch_one, preferred_element_type=jnp.float32)
    grad_attn_bf = (
        jnp.dot(grad_branch_one, full_attn.T, preferred_element_type=jnp.float32)
        .astype(jnp.bfloat16)
        .reshape(seqs, group, heads, HD)
    )
    delta = jnp.einsum("sqhd,shqd->shq", grad_attn_bf.astype(jnp.float32), attn_heads)
    kv_all = lax.all_gather(kv_local, "seq", axis=1, tiled=True)
    grad_queries = query_grads(kv_all, queries, grad_attn_bf, logsum, delta, width, factor)
    grad_kv = jnp.transpose(
        lax.psum_scatter(
            key_grads(
                kv_all,
                queries,
                grad_attn_bf,
                logsum,
                delta,
                width,
                factor,
                group * lax.axis_size("seq"),
            ).astype(jnp.bfloat16),
            "seq",
            scatter_dimension=0,
            tiled=True,
        ).astype(jnp.float32),
        (1, 0, 2),
    )
    grad_keys = grad_kv[..., :width].reshape(seqs, group, heads, HD)
    grad_qkv = jnp.concatenate(
        [
            rotate_back(grad_queries, cosines, sines).reshape(seqs, group, width),
            rotate_back(grad_keys, cosines, sines).reshape(seqs, group, width),
            grad_kv[..., width:],
        ],
        axis=-1,
    )
    grad_qkv = grad_qkv.astype(jnp.bfloat16).reshape(flat_rows, 3 * width)
    grad_w_qkv = jnp.dot(hidden_one.T, grad_qkv, preferred_element_type=jnp.float32)
    grad_hidden_one = jnp.dot(grad_qkv, full_qkv.T, preferred_element_type=jnp.float32).reshape(
        seqs, group, width
    )
    grad_shift_one, grad_scale_one, grad_gain_one, grad_normed_one = mod_back(
        grad_hidden_one, ln_one, normed_one, scale_one, vectors[0]
    )
    grad_start = grad_mid + norm_back(normed_one, inv_one, grad_normed_one)
    grad_mask_row = jnp.sum(jnp.where(masked[..., None], grad_start, 0.0), axis=(0, 1))
    grad_input = jnp.where(masked[..., None], 0.0, grad_start)
    grad_mod = jnp.concatenate(
        [
            grad_shift_one,
            grad_scale_one,
            grad_gate_one,
            grad_shift_two,
            grad_scale_two,
            grad_gate_two,
        ],
        axis=1,
    )
    grad_w_ada = jnp.dot(cond_bf.astype(jnp.float32).T, grad_mod, precision=lax.Precision.HIGHEST)
    grad_vectors = jnp.concatenate(
        [
            grad_gain_one[None, :],
            grad_gain_two[None, :],
            jnp.sum(grad_mod, axis=0).reshape(6, width),
            grad_mask_row[None, :],
        ],
        axis=0,
    )
    red_ada, red_qkv, red_attn, red_in, red_out, red_vec = (
        lax.psum_scatter(grad_w_ada, ("dp", "seq"), scatter_dimension=1, tiled=True),
        lax.psum_scatter(grad_w_qkv, ("dp", "seq"), scatter_dimension=0, tiled=True),
        lax.psum_scatter(grad_w_attn, ("dp", "seq"), scatter_dimension=0, tiled=True),
        lax.psum_scatter(grad_w_in, ("dp", "seq"), scatter_dimension=0, tiled=True),
        lax.psum_scatter(grad_w_out, ("dp", "seq"), scatter_dimension=0, tiled=True),
        lax.psum_scatter(grad_vectors, ("dp", "seq"), scatter_dimension=1, tiled=True),
    )
    local_squares = jnp.float32(0.0)
    for reduced in (red_vec, red_ada, red_qkv, red_attn, red_in, red_out):
        local_squares = local_squares + jnp.sum(reduced * reduced)
    grad_norm = jnp.sqrt(lax.psum(local_squares, ("dp", "seq")))
    clip_factor = jnp.minimum(1.0, CLIP / (grad_norm + 1e-06))
    columns = red_vec.shape[1]
    own_vectors = lax.dynamic_slice_in_dim(
        vectors, lax.axis_index(("dp", "seq")) * columns, columns, 1
    )
    vec_out = adam_step(own_vectors, red_vec * clip_factor, m_vec, v_vec, RATE_VECTORS, 0.0)
    ada_out = adam_step(w_ada, red_ada * clip_factor, m_ada, v_ada, RATE, DECAY)
    qkv_out = adam_step(w_qkv, red_qkv * clip_factor, m_qkv, v_qkv, RATE, DECAY)
    attn_out = adam_step(w_attn, red_attn * clip_factor, m_attn, v_attn, RATE, DECAY)
    in_out = adam_step(w_in, red_in * clip_factor, m_in, v_in, RATE, DECAY)
    out_out = adam_step(w_out, red_out * clip_factor, m_out, v_out, RATE, DECAY)
    return (
        block_out,
        grad_input,
        grad_norm,
        vec_out[0],
        vec_out[1],
        vec_out[2],
        ada_out[0],
        ada_out[1],
        ada_out[2],
        qkv_out[0],
        qkv_out[1],
        qkv_out[2],
        attn_out[0],
        attn_out[1],
        attn_out[2],
        in_out[0],
        in_out[1],
        in_out[2],
        out_out[0],
        out_out[1],
        out_out[2],
    )


F32, BF = jnp.float32, jnp.bfloat16
MESH = pl.DeviceIdType.MESH
DP, LINE, SEQ, CHIPS, ALL = 4, 4, 8, 16, 32
ROWS, WIDTH, PACK = 128, 768, 640
HALF = WIDTH // 2
HALVES = ((0, 0), (0, 1), (0, 2), (2, 2), (1, 0), (1, 1), (1, 2), None, (2, 0), (2, 1))

def numbered(**counts):
    at = {}
    for name, count in counts.items():
        at[name] = sum(counts[other] for other in at)
    return SimpleNamespace(**at), sum(counts.values())


S, SEM_COUNT = numbered(
    load=11,
    cond=1,
    mix_qkv=1,
    mix_in=1,
    mix_attn=1,
    mod=1,
    w_qkv=1,
    w_attn=1,
    plane_in=1,
    w_in=4,
    w_out=4,
    group_qkv=4,
    group_attn=4,
    fw_qkv=1,
    fw_attn=1,
    fw_in=1,
    fw_out=1,
    tok=4,
    h2=4,
    dm=4,
    xf=4,
    o=1,
    mm=1,
    dh2=1,
    do=1,
    gp=1,
    dh1=5,
    pair_out=1,
    pair_in=1,
    pair_attn=1,
    pair_qkv=1,
    plane_attn=1,
    plane_qkv=1,
    line_out=5,
    line_in=5,
    slice_in=1,
    line_attn=1,
    line_qkv=1,
    last_in=1,
    last_attn=1,
    last_qkv=1,
    early=1,
    early2=1,
    late=1,
    late2=1,
    sq=1,
)

SCRATCH = dict(
    i_tok=((1, 128, 768), BF),
    i_cot=((1, 128, 768), BF),
    i_vec=((9, 768), F32),
    i_wada=((144, 128), F32),
    i_wqkv=((24, 2304), F32),
    i_wattn=((24, 768), F32),
    i_win=((24, 3072), F32),
    i_wout=((96, 768), F32),
    wide_qkv=((48, 3072), F32),
    wide_in=((48, 3072), F32),
    wide_attn=((48, 768), F32),
    s_qkv=((48, 3072), BF),
    s_in=((48, 3072), BF),
    s_attn=((48, 768), BF),
    w_qkv=((768, 768), BF),
    w_in=((4, 4, 48, 768), BF),
    w_attn=((768, 768), BF),
    w_out=((4, 2, 96, 768), BF),
    t_w_qkv=((640, 768), BF),
    t_w_attn=((768, 1024), BF),
    t_w_in=((768, 768), BF),
    t_w_out=((768, 768), BF),
    t_h1=((768, 512), BF),
    conds_all=((4, 8, 128), F32),
    mod_send=((4, 4, 128), F32),
    mod_got=((32, 4, 128), F32),
    mod_flat=((40, 128), F32),
    mod_pad=((8, 384), F32),
    turn=((2, 4, 128, 128), F32),
    dmod_flat=((4, 40, 128), F32),
    mod=((8, 768), F32),
    x0=((128, 768), F32),
    n1=((128, 768), F32),
    inv1=((128, 128), F32),
    x1=((128, 768), F32),
    n2=((128, 768), F32),
    inv2=((128, 128), F32),
    a=((128, 768), F32),
    dx1=((128, 768), F32),
    toks=((4, 128, 768), BF),
    h1=((4, 128, 768), BF),
    h2=((4, 128, 768), BF),
    dm=((4, 128, 768), BF),
    gb=((4, 128, 768), BF),
    du=((4, 128, 768), BF),
    xb=((2, 4, 128, 640), BF),
    pt=((3, 1024, 512), BF),
    vt=((2, 128, 1024), BF),
    kt=((2, 128, 1024), BF),
    back=((4, 128, 768), F32),
    ot=((2, 128, 512), F32),
    os=((4, 192, 128), BF),
    ob=((4, 192, 128), BF),
    o2=((4, 128, 128), BF),
    mms=((4, 128, 768), BF),
    mmr=((4, 128, 768), BF),
    dhs=((4, 128, 768), BF),
    dhr=((4, 128, 768), BF),
    das=((128, 768), BF),
    dos=((4, 192, 128), BF),
    dob=((4, 192, 128), BF),
    dst=((3, 1024, 512), BF),
    ga=((512, 640), F32),
    gps=((512, 512), BF),
    gpr=((512, 512), BF),
    dqkv=((4, 128, 768), BF),
    d1s=((4, 128, 768), BF),
    d1r=((4, 128, 768), BF),
    g_out=((4, 2, 96, 768), BF),
    g_in=((2, 4, 4, 48, 384), BF),
    g_attn=((2, 768, 384), BF),
    g_qkv=((2, 768, 384), BF),
    p_out=((4, 96, 768), BF),
    p_in=((4, 4, 48, 384), BF),
    p_attn=((768, 384), BF),
    p_qkv=((768, 384), BF),
    q_attn=((4, 192, 384), BF),
    q_qkv=((4, 192, 384), BF),
    m_attn=((192, 384), BF),
    m_qkv=((192, 384), BF),
    r_out=((4, 96, 768), BF),
    r_in=((4, 4, 48, 384), BF),
    via_in=((4, 48, 384), BF),
    via_out=((96, 768), BF),
    via_dh1=((128, 768), BF),
    m_in=((4, 48, 384), BF),
    u_in=((4, 48, 384), BF),
    r_attn=((4, 48, 384), BF),
    r_qkv=((4, 48, 384), BF),
    t_in=((4, 48, 384), F32),
    t_attn=((1, 48, 384), F32),
    t_qkv=((4, 48, 384), F32),
    f_in=((4, 2, 24, 384), F32),
    f_attn=((1, 2, 24, 384), F32),
    f_qkv=((4, 2, 24, 384), F32),
    early=((8, 768), F32),
    early_got=((8, 8, 768), F32),
    early_all=((4, 8, 768), F32),
    late=((4, 768), F32),
    late_got=((8, 4, 768), F32),
    late_all=((4, 4, 768), F32),
    sq=((32, 1, 128), F32),
)


def dot(left, right):
    return jnp.dot(left, right, preferred_element_type=F32)


def dot_nt(left, right):
    return lax.dot_general(left, right, (((1,), (1,)), ((), ())), preferred_element_type=F32)


def dot_tn(left, right):
    return lax.dot_general(left, right, (((0,), (0,)), ((), ())), preferred_element_type=F32)


def loop(count, body, start=0):
    def step(index, carry):
        body(index)
        return carry

    lax.fori_loop(start, count, step, 0)


def layer_kernel(
    i_time,
    i_start,
    i_len,
    h_tok,
    h_cot,
    h_vec,
    h_wada,
    h_wqkv,
    h_wattn,
    h_win,
    h_wout,
    o_y,
    o_dx,
    o_norm,
    o_gqkv,
    o_gattn,
    o_gin,
    o_gout,
    o_dmod,
    o_gvec,
    o_vec,
    o_conds,
    *scratch,
):
    r = SimpleNamespace(**dict(zip(SCRATCH, scratch)), when=scratch[-3])
    send_sems, recv_sems = scratch[-2:]
    i_tok, i_cot, i_vec, i_wada = r.i_tok, r.i_cot, r.i_vec, r.i_wada
    i_wqkv, i_wattn, i_win, i_wout = r.i_wqkv, r.i_wattn, r.i_win, r.i_wout
    b, s = lax.axis_index("dp"), lax.axis_index("seq")
    z, c = lax.div(s, 2), lax.rem(s, 2)
    mate = s + 1 - 2 * c
    chip = b * LINE + z
    me = b * SEQ + s
    drains = []

    def push(src, dst, at, to_b, to_s, out=None):
        pltpu.make_async_remote_copy(
            src_ref=src,
            dst_ref=dst,
            send_sem=send_sems.at[at if out is None else out],
            recv_sem=recv_sems.at[at],
            device_id=(to_b, to_s),
            device_id_type=MESH,
        ).start()

    def keep(src, dst, at):
        pltpu.make_async_copy(src, dst, recv_sems.at[at]).start()

    def got(at, like):
        pltpu.make_async_copy(like, like, recv_sems.at[at]).wait()

    def left(at, like):
        pltpu.make_async_copy(like, like, send_sems.at[at]).wait()

    def sent(at, like):
        drains.append((at, like))

    near = (b, b + 1 - 2 * lax.rem(b, 2), b + 2 - 4 * lax.div(b, 2), 3 - b)

    def toward(k):
        if k == 3:
            return 3, near[3]
        slot = 1 + c if k == 1 else 2 - c
        return slot, (1 - c) * near[k] + c * near[3 - k]

    def peers(body):
        for k in (1, 2, 3):
            body(*toward(k))

    def stack(body):
        for k in (1, 2, 3):
            body(lax.rem(z + k + 2 * c * (2 - k), LINE))

    def line_gather(block, at, near=True, rest=True):
        inner = 1 + lax.rem(z, 2)
        if near:
            push(block(z), block(z), at + z, b, 2 * inner + c, at)

        def one(to):
            relayed = ((z == 1) & (to == 3)) | ((z == 2) & (to == 0))

            @pl.when(jnp.logical_not(relayed | (to == inner)))
            def _():
                push(block(z), block(z), at + z, b, 2 * to + c, at)

        if rest:
            stack(one)

    def line_relay(block, at):
        for middle, source, to in ((2, 1, 3), (1, 2, 0)):

            @pl.when(z == middle)
            def _():
                got(at + source, block(source))
                push(block(source), block(source), at + source, b, 2 * to + c, at)

    def line_got(block, at, k):
        here = (k == z) | ((z == 2) & (k == 1)) | ((z == 1) & (k == 2))

        @pl.when(jnp.logical_not(here))
        def _():
            got(at + k, block(0))

    far = lax.div(z, 2)

    def line_order(j):
        return lax.rem(z + (2, 3 - 2 * far, 1 + 2 * far, 0)[j], LINE)

    def line_add(j, rows, dst, via, at):
        to = line_order(j)
        outer_chip = (z == 0) | (z == 3)

        def direct():
            push(rows(to), dst.at[z], at + z, b, 2 * to + c, at)

        if j == 0:

            @pl.when(outer_chip)
            def _():
                push(rows(to), via, at + 4, b, 2 * (1 + far) + c, at)

            @pl.when(jnp.logical_not(outer_chip))
            def _():
                direct()

        elif j < 3:
            direct()
        else:
            keep(rows(z), dst.at[z], at + z)

    def line_via(via, at, add):
        @pl.when((z == 1) | (z == 2))
        def _():
            got(at + 4, via)
            add()

    def line_done(dst, at):
        for k in range(4):
            missing = ((z == 1) & (k == 3)) | ((z == 2) & (k == 0))

            @pl.when(jnp.logical_not(missing))
            def _():
                got(at + k, dst.at[k])

    def line_clear(dst):
        for middle, k in ((1, 3), (2, 0)):

            @pl.when(z == middle)
            def _():
                dst[k] = jnp.zeros(dst.shape[1:], BF)

    lane = lax.broadcasted_iota(jnp.int32, (1, 128), 1)
    low = lane < 64
    own24 = pl.ds(pl.multiple_of(24 * c, 8), 24)
    mate24 = pl.ds(pl.multiple_of(24 * (1 - c), 8), 24)
    part = pl.ds(pl.multiple_of(HALF * c, 128), HALF)
    chip_rows = pl.ds(pl.multiple_of(48 * chip, 16), 48)
    group_rows = pl.ds(pl.multiple_of(192 * b, 16), 192)

    barrier = pltpu.get_barrier_semaphore()

    def greet(k):
        other = lax.rem(me + k, ALL)
        pl.semaphore_signal(
            barrier, inc=1, device_id=(lax.div(other, SEQ), lax.rem(other, SEQ)), device_id_type=MESH
        )

    loads = (
        (i_time, r.when.at[0]),
        (i_start, r.when.at[1]),
        (i_len, r.when.at[2]),
        (h_wqkv, i_wqkv),
        (h_win, i_win),
        (h_wattn, i_wattn),
        (h_wout, i_wout),
        (h_tok, i_tok),
        (h_vec, i_vec),
        (h_wada, i_wada),
        (h_cot, i_cot),
    )
    for k, (src, dst) in enumerate(loads):
        pltpu.make_async_copy(src, dst, recv_sems.at[S.load + k]).start()
    loop(ALL, greet, 1)
    for k, (src, dst) in enumerate(loads):
        pltpu.make_async_copy(src, dst, recv_sems.at[S.load + k]).wait()

    def natural(kind, p, head):
        return kind * WIDTH + 192 * p + 64 * head

    def half_at(ref, column, high):
        tile = ref[:, column // 128 * 128 : column // 128 * 128 + 128]
        return tile if (column % 128 == 64) == high else pltpu.roll(tile, 64, 1)

    for p in range(4):
        for tile in range(5):
            pair = []
            for high in (0, 1):
                which = HALVES[2 * tile + high]
                pair.append(
                    jnp.zeros((24, 128), F32)
                    if which is None
                    else half_at(i_wqkv, natural(which[0], p, which[1]), bool(high))
                )
            r.wide_qkv[own24, 768 * p + 128 * tile : 768 * p + 128 * tile + 128] = jnp.where(
                low, pair[0], pair[1]
            )
        r.wide_qkv[own24, 768 * p + 640 : 768 * p + 768] = jnp.zeros((24, 128), F32)
    r.wide_in[own24, :] = i_win[...]
    r.wide_attn[own24, :] = i_wattn[...]
    r.w_out[z, c] = i_wout[...].astype(BF)
    r.toks[z] = i_tok[0]
    line_clear(r.r_out)
    line_clear(r.r_in)
    line_clear(r.d1r)
    lanes8 = lax.broadcasted_iota(jnp.int32, (8, 128), 1)
    half_cond = COND // 2
    speed = jnp.exp((lanes8 % half_cond).astype(F32) * (-math.log(10000.0) / half_cond))
    angle = r.when[0, 0].astype(F32) * speed
    wave = jnp.where(lanes8 < half_cond, jnp.cos(angle), jnp.sin(angle))
    r.conds_all[b] = wave * (1.0 / (1.0 + jnp.exp(-wave)))
    pl.semaphore_wait(barrier, ALL - 1)

    def token_block(k):
        return r.toks.at[k]

    def in_block(k):
        return r.w_in.at[:, k, :, part]

    def out_block(k):
        return r.w_out.at[k, c]

    peers(lambda k, to: push(r.conds_all.at[b], r.conds_all.at[b], S.cond, to, s))
    sent(S.cond, r.conds_all.at[0:3])
    push(r.wide_qkv.at[own24], r.wide_qkv.at[own24], S.mix_qkv, b, mate)
    sent(S.mix_qkv, r.wide_qkv.at[0:24])
    push(r.wide_attn.at[own24], r.wide_attn.at[own24], S.mix_attn, b, mate)
    sent(S.mix_attn, r.wide_attn.at[0:24])
    push(r.wide_in.at[own24], r.wide_in.at[own24], S.mix_in, b, mate)
    sent(S.mix_in, r.wide_in.at[0:24])

    got(S.cond, r.conds_all.at[0:3])
    row8 = lax.broadcasted_iota(jnp.int32, (8, 128), 0)
    cond4 = jnp.zeros((8, 128), F32)
    for k in range(4):
        cond4 = jnp.where(row8 == k, r.conds_all[k], cond4)
    o_conds[...] = cond4
    wide = i_wada.shape[0]
    r.mod_pad[...] = jnp.zeros((8, 384), F32)
    r.mod_pad[:, 0:wide] = dot_nt(cond4.astype(BF), i_wada[...].astype(BF))
    columns = pltpu.roll(r.mod_pad[...], lax.rem(wide * me, 128), 1)
    for k in range(4):
        for t in range(3):
            r.mod_send[k, t : t + 1, :] = columns[k : k + 1, 128 * t : 128 * t + 128]
        r.mod_send[k, 3:4, :] = jnp.zeros((1, 128), F32)

    def send_mod(k):
        other = lax.rem(me + k, ALL)
        ob = lax.div(other, SEQ)
        push(r.mod_send.at[ob], r.mod_got.at[me], S.mod, ob, lax.rem(other, SEQ))

    loop(ALL, send_mod, 1)
    sent(S.mod, r.mod_got.at[0:31])
    keep(r.mod_send.at[b], r.mod_got.at[me], S.mod)

    def block(src, first):
        return src.at[:, pl.ds(pl.multiple_of(first, 128), HALF)]

    def along_line(src, dst, at, step):
        stack(
            lambda to: push(
                block(src, step * to + HALF * c), dst.at[chip_rows, part], at, b, 2 * to + c
            )
        )
        keep(block(src, step * z + HALF * c), dst.at[chip_rows, part], at)
        sent(at, dst.at[0:144, 0:HALF])

    def over_plane(dst, first, at):
        got(first, dst.at[0:192, 0:HALF])
        rows = dst.at[group_rows, part]
        peers(lambda k, to: push(rows, rows, at + k, to, s))
        for k in (1, 2, 3):
            sent(at + k, dst.at[0:192, 0:HALF])

    def share(dst, at, onward):
        for k in range(4):
            rows = dst.at[pl.ds(pl.multiple_of(192 * near[k], 16), 192), part]
            if k:
                got(at + k, rows)
            push(rows, rows, onward, b, mate)
        sent(onward, dst.at[:, 0:HALF])

    def line_share(block, at, onward):
        for k in range(4):
            line_got(block, at, k)
            push(block(k), block(k), onward, b, mate)

    got(S.mix_qkv, r.wide_qkv.at[0:24])
    r.s_qkv[...] = r.wide_qkv[...].astype(BF)
    along_line(r.s_qkv, r.w_qkv, S.w_qkv, WIDTH)
    line_gather(token_block, S.tok, rest=False)
    sent(S.tok, r.toks.at[0:3])
    got(S.mix_attn, r.wide_attn.at[0:24])
    r.s_attn[...] = r.wide_attn[...].astype(BF)
    over_plane(r.w_qkv, S.w_qkv, S.group_qkv)
    line_gather(token_block, S.tok, near=False)
    along_line(r.s_attn, r.w_attn, S.w_attn, 0)
    line_gather(out_block, S.w_out)
    sent(S.w_out, r.w_out.at[0:3, 0])
    got(S.mix_in, r.wide_in.at[0:24])
    r.s_in[...] = r.wide_in[...].astype(BF)
    peers(
        lambda k, to: push(
            block(r.s_in, WIDTH * to + HALF * c), r.w_in.at[b, z, :, part], S.plane_in, to, s
        )
    )
    keep(block(r.s_in, WIDTH * b + HALF * c), r.w_in.at[b, z, :, part], S.plane_in)
    sent(S.plane_in, r.w_in.at[0:3, 0, :, 0:HALF])

    def start_tokens(tokens, k):
        place = (2 * k + c) * ROWS + lax.broadcasted_iota(jnp.int32, (ROWS, 1), 0)
        hidden = (place >= r.when[1, 0]) & (place < r.when[1, 0] + r.when[2, 0])
        return jnp.where(hidden, i_vec[8:9, :], tokens.astype(F32)), hidden

    x0, _ = start_tokens(i_tok[0], z)
    r.x0[...] = x0
    n1, inv1 = normalize(x0)
    r.n1[...] = n1
    r.inv1[...] = jnp.broadcast_to(inv1, (ROWS, 128))

    got(S.mod, r.mod_got)
    r.mod_flat[...] = jnp.zeros((40, 128), F32)
    for k in range(ALL):
        first = 9 * k // 8
        r.mod_flat[first : first + 3, :] += r.mod_got[k, 0:3, :]
    for k in range(6):
        row = jnp.concatenate(
            [r.mod_flat[6 * k + t : 6 * k + t + 1, :] for t in range(6)], axis=1
        )
        r.mod[k : k + 1, :] = row + i_vec[2 + k : 3 + k, :]

    def mod(k):
        return r.mod[k : k + 1, :]

    def vec(k):
        return i_vec[k : k + 1, :]

    r.h1[z] = (r.n1[...] * vec(0) * (1.0 + mod(1)) + mod(0)).astype(BF)
    r.dm[0] = (i_cot[0].astype(F32) * mod(5)).astype(BF)
    peers(lambda k, to: push(r.dm.at[0], r.dm.at[k], S.dm + k, to, s))
    for k in (1, 2, 3):
        sent(S.dm + k, r.dm.at[0])

    lanes = lax.broadcasted_iota(jnp.int32, (ROWS, 128), 1)
    first_half = lanes % HD < HD // 2
    speed = jnp.exp((lanes % (HD // 2)).astype(F32) * (-math.log(10000.0) / (HD // 2)))
    row = lax.broadcasted_iota(jnp.int32, (ROWS, 128), 0)

    def table(k):
        angle = ((2 * k + c) * ROWS + row).astype(F32) * speed
        r.turn[0, k] = jnp.cos(angle)
        sine = jnp.sin(angle)
        r.turn[1, k] = jnp.where(first_half, -sine, sine)

    loop(LINE, table)

    line_relay(token_block, S.tok)

    share(r.w_qkv, S.group_qkv, S.fw_qkv)
    got(S.fw_qkv, r.w_qkv.at[:, 0:HALF])
    for k in range(5):
        columns = slice(128 * k, 128 * k + 128)
        r.t_w_qkv[columns, :] = r.w_qkv[:, columns].T

    def turned(tile, sign, k):
        other = jnp.where(first_half, pltpu.roll(tile, 96, 1), pltpu.roll(tile, 32, 1))
        return tile * r.turn[0, k] + sign * (other * r.turn[1, k])

    def project(j):
        k = lax.rem(z + j, LINE)

        @pl.when(j > 0)
        def _():
            line_got(token_block, S.tok, k)
            other, _ = start_tokens(r.toks[k], k)
            other, _ = normalize(other)
            r.h1[k] = (other * vec(0) * (1.0 + mod(1)) + mod(0)).astype(BF)

        x = dot(r.h1[k], r.w_qkv[:, 0:PACK])
        tiles = [x[:, 128 * t : 128 * t + 128] for t in range(5)]
        tiles[0] = turned(tiles[0], 1.0, k) * 0.125
        tiles[1] = jnp.where(low, turned(tiles[1], 1.0, k) * 0.125, tiles[1])
        tiles[2] = turned(tiles[2], 1.0, k)
        tiles[3] = turned(tiles[3], 1.0, k)
        for t in range(5):
            r.xb[0, k, :, 128 * t : 128 * t + 128] = tiles[t].astype(BF)
        push(r.xb.at[0, k], r.xb.at[1, k], S.xf + k, b, mate)

    loop(4, project)
    over_plane(r.w_attn, S.w_attn, S.group_attn)
    for k in range(4):
        sent(S.xf + k, r.xb.at[0, 0])

    for k in range(4):
        got(S.xf + k, r.xb.at[0, 0])

    def tile_of(t):
        return r.xb[:, :, :, 128 * t : 128 * t + 128].reshape(1024, 128)

    heads = ((0, 2, 4, True, True), (0, 2, 4, False, False), (1, 3, 1, True, False))

    def queries(head, first, size):
        q_tile, _, _, q_low, _ = heads[head]
        q = r.xb[0, first : first + size, :, 128 * q_tile : 128 * q_tile + 128]
        return jnp.where(low if q_low else ~low, q.reshape(size * 128, 128), jnp.zeros((), BF))

    r.vt[0] = tile_of(4).T
    r.vt[1] = tile_of(1).T
    for half in range(2):
        at = slice(256 * half, 256 * half + 256)
        for head in range(3):
            scores = dot_nt(tile_of(heads[head][1]), queries(head, 2 * half, 2))
            weights = jnp.exp(scores - jnp.max(scores, axis=0, keepdims=True))
            weights = weights * (1.0 / jnp.sum(weights, axis=0, keepdims=True))
            weights = weights.astype(BF)
            r.pt[head, :, at] = weights
            out = dot(r.vt[head // 2], weights)
            if head == 0:
                r.ot[0, 0:64, at] = out[0:64]
            elif head == 1:
                r.ot[0, 64:128, at] = out[64:128]
            else:
                r.ot[1, 0:64, at] = out[64:128]
                r.ot[1, 64:128, at] = jnp.zeros((64, 256), F32)
        for k in (2 * half, 2 * half + 1):
            across = slice(128 * k, 128 * k + 128)
            r.os[k, 0:128, :] = r.ot[0, :, across].T.astype(BF)
            third = r.ot[1, 0:64, across]
            third = jnp.concatenate([third, pltpu.roll(third, 64, 1)], axis=0)
            r.os[k, 128:192, :] = third.T[0:64].astype(BF)
        for to in (2 * half, 2 * half + 1):

            @pl.when(z == to)
            def _():
                keep(r.os.at[to], r.ob.at[z], S.o)

            @pl.when(z != to)
            def _():
                push(r.os.at[to], r.ob.at[z], S.o, b, 2 * to + c)

        if half == 0:
            line_relay(out_block, S.w_out)

    sent(S.o, r.os.at[0:3])
    got(S.plane_in, r.w_in.at[:, 0, :, 0:HALF])
    line_gather(in_block, S.w_in)
    sent(S.w_in, r.w_in.at[0:3, :, :, 0:HALF])
    for k in range(2):
        r.kt[k] = tile_of(2 + k).T
    share(r.w_attn, S.group_attn, S.fw_attn)
    got(S.fw_attn, r.w_attn.at[:, 0:HALF])
    for p in range(4):
        first = 192 * p
        r.t_w_attn[:, 256 * p : 256 * p + 128] = r.w_attn[first : first + 128, :].T
        third = r.w_attn[first + 128 : first + 192, :]
        r.t_w_attn[:, 256 * p + 128 : 256 * p + 256] = jnp.concatenate(
            [third, jnp.zeros_like(third)], axis=0
        ).T
    got(S.o, r.ob)
    a = jnp.zeros((ROWS, WIDTH), F32)
    for p in range(4):
        third = r.ob[p, 128:192, :].astype(F32)
        third = jnp.concatenate([third, pltpu.roll(third, 64, 1)], axis=0)
        r.o2[p] = jnp.where(low, third, 0.0).astype(BF)
        a += dot(r.ob[p, 0:128, :], r.w_attn[192 * p : 192 * p + 128, :])
        a += dot(r.o2[p, :, 0:64], r.w_attn[192 * p + 128 : 192 * p + 192, :])
    r.a[...] = a
    x1 = r.x0[...] + mod(2) * a
    r.x1[...] = x1
    n2, inv2 = normalize(x1)
    r.n2[...] = n2
    r.inv2[...] = jnp.broadcast_to(inv2, (ROWS, 128))
    r.h2[0] = (n2 * vec(1) * (1.0 + mod(4)) + mod(3)).astype(BF)
    peers(lambda k, to: push(r.h2.at[0], r.h2.at[k], S.h2 + k, to, s))
    for k in (1, 2, 3):
        sent(S.h2 + k, r.h2.at[0])
    line_relay(in_block, S.w_in)
    line_share(out_block, S.w_out, S.fw_out)
    sent(S.fw_out, r.w_out.at[:, 0])
    got(S.fw_out, r.w_out.at[:, 0])

    for k in range(6):
        columns = slice(128 * k, 128 * k + 128)
        r.t_w_out[columns, :] = r.w_out[:, :, :, columns].reshape(WIDTH, 128).T

    def feed_back(k):
        @pl.when(k > 0)
        def _():
            got(S.dm + k, r.dm.at[0])

        r.back[k] = dot(r.dm[k], r.t_w_out[...])

    loop(4, feed_back)
    line_share(in_block, S.w_in, S.fw_in)
    sent(S.fw_in, r.w_in.at[:, :, :, 0:HALF])
    got(S.fw_in, r.w_in.at[:, :, :, 0:HALF])
    for k in range(6):
        columns = slice(128 * k, 128 * k + 128)
        r.t_w_in[columns, :] = r.w_in[:, :, :, columns].reshape(WIDTH, 128).T

    def feed(first, count):
        at = slice(first, first + count)
        size = count * ROWS
        u = dot(r.h2[at].reshape(size, WIDTH), r.w_in[...].reshape(WIDTH, WIDTH))
        slope = 0.7978845608028654
        cube = 0.044715
        t = jnp.tanh(slope * (u + cube * u * u * u))
        r.gb[at] = (0.5 * u * (1.0 + t)).astype(BF).reshape(count, ROWS, WIDTH)
        bend = 0.5 * (1.0 + t) + 0.5 * u * (1.0 - t * t) * (slope * (1.0 + 3.0 * cube * u * u))
        du = (r.back[at].reshape(size, WIDTH) * bend).astype(BF)
        r.du[at] = du.reshape(count, ROWS, WIDTH)
        r.dhs[at] = dot(du, r.t_w_in[...]).astype(BF).reshape(count, ROWS, WIDTH)

    feed(0, 1)
    for first, count in ((1, 2), (3, 1)):
        for k in range(first, first + count):
            got(S.h2 + k, r.h2.at[0])
        feed(first, count)
        for k in range(first, first + count):
            slot, to = toward(k)
            push(r.dhs.at[slot], r.dhr.at[slot], S.dh2, to, s)
    sent(S.dh2, r.dhs.at[0:3])
    def gather(own, others):
        total = own[0].astype(F32)
        for k in (1, 2, 3):
            total += others[k].astype(F32)
        return total

    for k in range(2):
        rows = slice(384 * k, 384 * k + 384)
        result = dot_tn(r.gb[:, :, rows].reshape(512, 384), r.dm[...].reshape(512, 768))
        r.g_out[2 * k : 2 * k + 2] = result.astype(BF).reshape(2, 2, 96, 768)
    push(r.g_out.at[:, 1 - c], r.p_out, S.pair_out, b, mate)
    sent(S.pair_out, r.p_out)

    def to_mate(grad, dst, at):
        push(grad.at[1 - c], dst, at, b, mate)
        sent(at, dst)

    def pair_sum(grad, pair, at):
        got(at, pair)
        grad[c] = (grad[c].astype(F32) + pair[...].astype(F32)).astype(BF)

    def plane_sum(grad, dst, at):
        def rows(to):
            return grad.at[c, pl.ds(pl.multiple_of(192 * to, 16), 192)]

        peers(lambda k, to: push(rows(to), dst.at[k], at, to, s))
        keep(rows(b), dst.at[0], at)
        sent(at, dst.at[0:3])

    def line_sum(src, total, dst, first, at):
        got(first, src)
        total[...] = (
            (src[0].astype(F32) + src[1].astype(F32)) + (src[2].astype(F32) + src[3].astype(F32))
        ).astype(BF)

        def rows(to):
            return total.at[pl.ds(pl.multiple_of(48 * to, 16), 48)]

        stack(lambda to: push(rows(to), dst.at[z], at, b, 2 * to + c))
        keep(rows(z), dst.at[z], at)
        sent(at, dst.at[0:3])

    def trade(total, final, at):
        push(total.at[:, mate24], final.at[:, c], at, b, mate)
        sent(at, final.at[:, 0])
        final[:, c] = total[:, own24, :]

    for k in range(2):
        rows = slice(384 * k, 384 * k + 384)
        result = dot_tn(r.h2[:, :, rows].reshape(512, 384), r.du[...].reshape(512, 768)).astype(BF)
        for h in range(2):
            r.g_in[h, 2 * k : 2 * k + 2] = result[:, 384 * h : 384 * h + 384].reshape(2, 4, 48, 384)
    to_mate(r.g_in, r.p_in, S.pair_in)

    got(S.pair_out, r.p_out)
    for k in range(4):
        r.g_out[k, c] = (r.g_out[k, c].astype(F32) + r.p_out[k].astype(F32)).astype(BF)

    def out_rows(k):
        return r.g_out.at[k, c]

    for j in (0, 1):
        line_add(j, out_rows, r.r_out, r.via_out, S.line_out)

    def add_out():
        k = line_order(2)
        r.g_out[k, c] = (r.g_out[k, c].astype(F32) + r.via_out[...].astype(F32)).astype(BF)

    got(S.dh2, r.dhr.at[0:3])
    dh = gather(r.dhs, r.dhr)
    n2 = r.n2[...]
    inv2 = r.inv2[:, 0:1]
    r.early[...] = jnp.zeros((8, 768), F32)
    r.early[2:3, :] = jnp.sum(dh, axis=0, keepdims=True)
    both = jnp.sum(dh * n2, axis=0, keepdims=True)
    r.early[3:4, :] = both * vec(1)
    r.early[0:1, :] = both * (1.0 + mod(4))
    grad = dh * ((1.0 + mod(4)) * vec(1))
    dx1 = i_cot[0].astype(F32) + norm_back(n2, inv2, grad)
    r.dx1[...] = dx1
    r.early[1:2, :] = jnp.sum(dx1 * r.a[...], axis=0, keepdims=True)
    r.das[...] = (dx1 * mod(2)).astype(BF)
    for p in range(4):
        result = dot(r.das[...], r.t_w_attn[:, 256 * p : 256 * p + 256])
        r.dos[p, 0:128, :] = result[:, 0:128].astype(BF)
        third = result[:, 128:256]
        third = jnp.where(low, third[0:64], pltpu.roll(third[64:128], 64, 1))
        r.dos[p, 128:192, :] = third.astype(BF)
    stack(lambda to: push(r.dos.at[to], r.dob.at[z], S.do, b, 2 * to + c))
    keep(r.dos.at[z], r.dob.at[z], S.do)
    sent(S.do, r.dos.at[0:3])
    for t in range(3):
        at = slice(256 * t, 256 * t + 256)
        mm = dot(r.gb[...].reshape(512, WIDTH), r.w_out[:, :, :, at].reshape(WIDTH, 256))
        r.mms[:, :, at] = mm.astype(BF).reshape(4, ROWS, 256)
    peers(lambda k, to: push(r.mms.at[k], r.mmr.at[k], S.mm, to, s))
    sent(S.mm, r.mms.at[0:3])

    for p in range(4):
        for rows, left_side in (
            (slice(192 * p, 192 * p + 128), r.ob[p, 0:128, :]),
            (slice(192 * p + 128, 192 * p + 192), r.o2[p]),
        ):
            result = dot_tn(left_side, r.das[...])[0 : rows.stop - rows.start].astype(BF)
            r.g_attn[0, rows, :] = result[:, 0:HALF]
            r.g_attn[1, rows, :] = result[:, HALF:WIDTH]
    to_mate(r.g_attn, r.p_attn, S.pair_attn)

    def over_line(src, dst, name):
        def one(k):
            push(src, dst.at[s], name, b, lax.rem(s + k, SEQ))

        loop(SEQ, one, 1)
        keep(src, dst.at[s], name)
        sent(name, dst.at[0:7])

    def over_group(got_ref, dst, name):
        total = got_ref[0]
        for k in range(1, SEQ):
            total += got_ref[k]
        dst[b] = total
        peers(lambda k, to: push(dst.at[b], dst.at[b], name, to, s))
        sent(name, dst.at[0:3])


    pair_sum(r.g_in, r.p_in, S.pair_in)

    line_via(r.via_out, S.line_out, add_out)
    for j in (2, 3):
        line_add(j, out_rows, r.r_out, r.via_out, S.line_out)
    sent(S.line_out, r.r_out.at[0:3])

    def in_rows(k):
        return r.g_in.at[c, :, k]

    for j in (0, 1):
        line_add(j, in_rows, r.r_in, r.via_in, S.line_in)

    def add_in():
        k = line_order(2)
        r.g_in[c, :, k] = (r.g_in[c, :, k].astype(F32) + r.via_in[...].astype(F32)).astype(BF)

    pair_sum(r.g_attn, r.p_attn, S.pair_attn)
    plane_sum(r.g_attn, r.q_attn, S.plane_attn)

    for k in range(6):
        columns = slice(128 * k, 128 * k + 128)
        r.t_h1[columns, :] = r.h1[:, :, columns].reshape(512, 128).T
    got(S.do, r.dob)
    dot0 = r.dob[:, 0:128, :].reshape(512, 128)
    third = r.dob[:, 128:192, :].astype(F32).reshape(256, 128)
    other_rows = jnp.where(low, pltpu.roll(third, 64, 1), 0.0).reshape(4, 64, 128)
    third = jnp.where(low, third, 0.0).reshape(4, 64, 128)
    dot1 = jnp.concatenate([third, other_rows], axis=1).reshape(512, 128)
    zero = jnp.zeros((), BF)
    moved = pltpu.roll(dot1, 64, 1).astype(BF)
    grads = (jnp.where(low, dot0, zero), jnp.where(low, zero, dot0), moved)
    product = dot0.astype(F32).T * r.ot[0]
    deltas = (
        jnp.sum(product[0:64], axis=0, keepdims=True),
        jnp.sum(product[64:128], axis=0, keepdims=True),
        jnp.sum(dot1.T * r.ot[1], axis=0, keepdims=True),
    )
    for head in range(3):
        values = tile_of(heads[head][2])
        for half in range(2):
            at = slice(256 * half, 256 * half + 256)
            dp = dot_nt(values, grads[head][at])
            r.dst[head, :, at] = (
                r.pt[head, :, at].astype(F32) * (dp - deltas[head][:, at])
            ).astype(BF)

    def key_grads(rows):
        dk = [dot(r.dst[head, rows, :], queries(head, 0, 4)) for head in range(3)]
        dv = [dot(r.pt[head, rows, :], grads[head]) for head in range(3)]
        return (dv[2], dk[0] + dk[1], dk[2], dv[0] + dv[1])

    line_via(r.via_in, S.line_in, add_in)
    for j in (2, 3):
        line_add(j, in_rows, r.r_in, r.via_in, S.line_in)
    sent(S.line_in, r.r_in.at[0:3])
    for t, tile in enumerate(key_grads(slice(512, 1024))):
        r.gps[:, 128 * t : 128 * t + 128] = tile.astype(BF)
    push(r.gps, r.gpr, S.gp, b, mate)
    sent(S.gp, r.gps)
    for t, tile in enumerate(key_grads(slice(0, 512))):
        r.ga[:, 128 * t + 128 : 128 * t + 256] = tile
    for half in range(2):
        at = slice(256 * half, 256 * half + 256)
        turned_q = [dot(r.kt[head // 2], r.dst[head, :, at]) for head in range(3)]
        top = jnp.concatenate([turned_q[0][0:64], turned_q[1][64:128]], axis=0)
        r.ga[at, 0:128] = top.T * 0.125
        r.ga[at, 128:256] += turned_q[2].T * 0.125
    got(S.mm, r.mmr.at[0:3])
    mm = gather(r.mms, r.mmr)
    o_y[...] = (r.x1[...] + mod(5) * mm).astype(BF)
    r.early[4:5, :] = jnp.sum(i_cot[0].astype(F32) * mm, axis=0, keepdims=True)
    over_line(r.early, r.early_got, S.early)
    got(S.gp, r.gpr)

    def dh1_rows(k):
        return r.d1s.at[k]

    def back_turn(k):
        rows = pl.ds(pl.multiple_of(128 * k, 128), 128)
        tiles = [r.ga[rows, 0:128]] + [
            r.ga[rows, 128 * t : 128 * t + 128]
            + r.gpr[rows, 128 * t - 128 : 128 * t].astype(F32)
            for t in range(1, 5)
        ]
        tiles[0] = turned(tiles[0], -1.0, k)
        tiles[1] = jnp.where(low, turned(tiles[1], -1.0, k), tiles[1])
        tiles[2] = turned(tiles[2], -1.0, k)
        tiles[3] = turned(tiles[3], -1.0, k)
        for t in range(5):
            r.dqkv[k, :, 128 * t : 128 * t + 128] = tiles[t].astype(BF)
        r.dqkv[k, :, PACK:WIDTH] = jnp.zeros((128, 128), BF)

    loop(4, back_turn)

    def unproject(j):
        k = line_order(j)
        partial_sum = dot(r.dqkv[k, :, 0:PACK], r.t_w_qkv[...])
        r.d1s[k] = partial_sum.astype(BF)
        if j == 2:

            def add():
                r.d1s[k] = (partial_sum + r.via_dh1[...].astype(F32)).astype(BF)

            line_via(r.via_dh1, S.dh1, add)
        line_add(j, dh1_rows, r.d1r, r.via_dh1, S.dh1)

    unproject(0)

    def qkv_rows(k):
        rows = pl.ds(pl.multiple_of(128 * k, 128), 128)
        result = dot(r.t_h1[rows, :], r.dqkv[...].reshape(512, WIDTH)).astype(BF)
        r.g_qkv[0, rows, :] = result[:, 0:HALF]
        r.g_qkv[1, rows, :] = result[:, HALF:WIDTH]

    loop(6, qkv_rows)
    to_mate(r.g_qkv, r.p_qkv, S.pair_qkv)
    unproject(1)
    pair_sum(r.g_qkv, r.p_qkv, S.pair_qkv)
    plane_sum(r.g_qkv, r.q_qkv, S.plane_qkv)
    unproject(2)
    unproject(3)
    sent(S.dh1, r.d1s.at[0:3])
    line_sum(r.q_attn, r.m_attn, r.r_attn, S.plane_attn, S.line_attn)
    got(S.early, r.early_got)
    over_group(r.early_got, r.early_all, S.early2)

    line_done(r.r_in, S.line_in)
    r.m_in[...] = (
        (r.r_in[0].astype(F32) + r.r_in[1].astype(F32))
        + (r.r_in[2].astype(F32) + r.r_in[3].astype(F32))
    ).astype(BF)
    peers(lambda k, to: push(r.m_in.at[to], r.u_in.at[b], S.slice_in, to, s))
    keep(r.m_in.at[b], r.u_in.at[b], S.slice_in)
    sent(S.slice_in, r.u_in.at[0:3])
    line_sum(r.q_qkv, r.m_qkv, r.r_qkv, S.plane_qkv, S.line_qkv)

    line_done(r.d1r, S.dh1)
    dh = (r.d1r[0].astype(F32) + r.d1r[1].astype(F32)) + (
        r.d1r[2].astype(F32) + r.d1r[3].astype(F32)
    )
    n1 = r.n1[...]
    both = jnp.sum(dh * n1, axis=0, keepdims=True)
    r.late[0:1, :] = both * (1.0 + mod(1))
    r.late[1:2, :] = jnp.sum(dh, axis=0, keepdims=True)
    r.late[2:3, :] = both * vec(0)
    grad = dh * ((1.0 + mod(1)) * vec(0))
    dx0 = r.dx1[...] + norm_back(n1, r.inv1[:, 0:1], grad)
    _, hidden = start_tokens(i_tok[0], z)
    o_dx[...] = jnp.where(hidden, 0.0, dx0)
    r.late[3:4, :] = jnp.sum(jnp.where(hidden, dx0, 0.0), axis=0, keepdims=True)
    over_line(r.late, r.late_got, S.late)

    line_done(r.r_out, S.line_out)
    total = (r.r_out[0].astype(F32) + r.r_out[1].astype(F32)) + (
        r.r_out[2].astype(F32) + r.r_out[3].astype(F32)
    )
    o_gout[...] = total
    squares = total * total
    squares = jnp.sum(squares[:, 0:128] + squares[:, 128:256] + squares[:, 256:384]
                      + squares[:, 384:512] + squares[:, 512:640] + squares[:, 640:768],
                      axis=0, keepdims=True)

    def fold(value):
        total = value[:, 0:128] * value[:, 0:128]
        for t in range(1, value.shape[1] // 128):
            total += value[:, 128 * t : 128 * t + 128] * value[:, 128 * t : 128 * t + 128]
        return jnp.sum(total, axis=0, keepdims=True)

    got(S.slice_in, r.u_in)
    r.t_in[...] = r.u_in[...].astype(F32)
    for p in range(4):
        squares += fold(r.t_in[p])
    trade(r.t_in, r.f_in, S.last_in)
    got(S.line_attn, r.r_attn)
    r.t_attn[0] = (r.r_attn[0].astype(F32) + r.r_attn[1].astype(F32)) + (
        r.r_attn[2].astype(F32) + r.r_attn[3].astype(F32)
    )
    squares += fold(r.t_attn[0])
    trade(r.t_attn, r.f_attn, S.last_attn)
    got(S.line_qkv, r.r_qkv)
    r.t_qkv[...] = r.r_qkv[...].astype(F32)
    trade(r.t_qkv, r.f_qkv, S.last_qkv)
    for p in range(4):
        squares += fold(r.t_qkv[p])
    r.sq[me] = squares

    def send_sq(k):
        other = lax.rem(me + k, ALL)
        push(r.sq.at[me], r.sq.at[me], S.sq, lax.div(other, SEQ), lax.rem(other, SEQ))

    loop(ALL, send_sq, 1)
    sent(S.sq, r.sq.at[0:31])
    got(S.late, r.late_got)
    over_group(r.late_got, r.late_all, S.late2)
    got(S.last_in, r.f_in.at[:, 0])
    got(S.last_attn, r.f_attn.at[:, 0])
    for h in range(2):
        for p in range(4):
            value = r.f_in[p, h]
            o_gin[:, 768 * p + 384 * h : 768 * p + 384 * h + 384] = value
        value = r.f_attn[0, h]
        o_gattn[:, 384 * h : 384 * h + 384] = value
    got(S.last_qkv, r.f_qkv.at[:, 0])
    where = {which: index for index, which in enumerate(HALVES) if which is not None}

    def packed_half(chunk, high):
        kind, rest = chunk // 12, chunk % 12
        index = where[(kind, rest % 3)]
        t = index // 2
        tile = r.f_qkv[rest // 3, t // 3, :, t % 3 * 128 : t % 3 * 128 + 128]
        return tile if index % 2 == high else pltpu.roll(tile, 64, 1)

    for t in range(18):
        o_gqkv[:, 128 * t : 128 * t + 128] = jnp.where(
            low, packed_half(2 * t, 0), packed_half(2 * t + 1, 1)
        )
    got(S.early2, r.early_all.at[0:3])
    got(S.late2, r.late_all.at[0:3])
    mods = []
    for k in range(4):
        early, late = r.early_all[k], r.late_all[k]
        rows = jnp.concatenate([late[1:3], early[1:5], jnp.zeros((2, 768), F32)], axis=0)
        for n in range(6):
            for m in range(6):
                r.dmod_flat[k, 6 * n + m : 6 * n + m + 1, :] = rows[
                    n : n + 1, 128 * m : 128 * m + 128
                ]
        mods.append(rows)
    gain = jnp.concatenate(
        [
            sum(r.late_all[k][0:1] for k in range(4)),
            sum(r.early_all[k][0:1] for k in range(4)),
            (mods[0] + mods[1] + mods[2] + mods[3])[0:6],
        ],
        axis=0,
    )
    mask_row = sum(r.late_all[k][3:4] for k in range(4))
    gains = jnp.concatenate([gain, mask_row, jnp.zeros((7, 768), F32)], axis=0)
    masters = jnp.concatenate([i_vec[...], jnp.zeros((7, 768), F32)], axis=0)
    own = lax.rem(WIDTH - 24 * me, WIDTH)
    o_gvec[...] = pltpu.roll(gains, own, 1)[:, 0:128]
    o_vec[...] = pltpu.roll(masters, own, 1)[:, 0:128]
    r.mod_pad[...] = jnp.zeros((8, 384), F32)
    window = lax.div(wide * me, 128)
    for k in range(4):
        rows = r.dmod_flat[k, pl.ds(window, 3), :]
        for m in range(3):
            r.mod_pad[k : k + 1, 128 * m : 128 * m + 128] = rows[m : m + 1, :]
    o_dmod[...] = pltpu.roll(r.mod_pad[...], lax.rem(384 - lax.rem(wide * me, 128), 384), 1)[:, 0:256]
    small = jnp.sum(gain * gain) + jnp.sum(mask_row * mask_row)
    conds = [r.conds_all[k][0:1].astype(BF).astype(F32) for k in range(4)]
    for k in range(4):
        for m in range(k, 4):
            term = jnp.sum(mods[k] * mods[m]) * jnp.sum(conds[k] * conds[m])
            small += term if m == k else 2.0 * term
    got(S.sq, r.sq.at[0:31])
    total = r.sq[0]
    for k in range(1, ALL):
        total += r.sq[k]
    o_norm[...] = jnp.broadcast_to(jnp.sqrt(jnp.sum(total) + small), (8, 128))

    for at, like in drains:
        left(at, like)


def run_layer(*args):
    shapes = (
        ((ROWS, WIDTH), BF),
        ((ROWS, WIDTH), F32),
        ((8, 128), F32),
        ((24, 3 * WIDTH), F32),
        ((24, WIDTH), F32),
        ((24, 4 * WIDTH), F32),
        ((96, WIDTH), F32),
        ((8, 256), F32),
        ((16, 128), F32),
        ((16, 128), F32),
        ((8, 128), F32),
    )
    whole = pl.BlockSpec(memory_space=pltpu.VMEM)
    return pl.pallas_call(
        layer_kernel,
        out_shape=[jax.ShapeDtypeStruct(shape, kind) for shape, kind in shapes],
        in_specs=[pl.BlockSpec(memory_space=pl.ANY)] * len(args),
        out_specs=[whole] * len(shapes),
        scratch_shapes=[pltpu.VMEM(shape, kind) for shape, kind in SCRATCH.values()]
        + [pltpu.SMEM((3, 1), jnp.int32)]
        + [pltpu.SemaphoreType.DMA((SEM_COUNT,)), pltpu.SemaphoreType.DMA((SEM_COUNT,))],
        compiler_params=pltpu.CompilerParams(
            collective_id=0, has_side_effects=True, vmem_limit_bytes=60 * 1024 * 1024
        ),
    )(*args)


def finish_kernel(
    y, dx, norm, g_qkv, g_attn, g_in, g_out, dmod, g_vec, own_vec, conds, *rest
):
    (w_ada, w_qkv, w_attn, w_in, w_out), moments, outs = rest[:5], rest[5:17], rest[17:]
    outs[0][0] = y[...]
    outs[1][0] = dx[...]
    outs[2][0, 0] = norm[0, 0]
    clip = jnp.minimum(1.0, CLIP / (norm[0:1, 0:1] + 1e-06))
    columns = w_ada.shape[0]
    rounded = conds[...].astype(BF).astype(F32)
    turned_mod = dmod[...].T
    g_ada = turned_mod[0:columns, 0:1] * rounded[0:1, :]
    for k in range(1, 4):
        g_ada += turned_mod[0:columns, k : k + 1] * rounded[k : k + 1, :]
    narrow = moments[0].shape[1]
    grads = (
        g_vec[0:9, 0:narrow],
        g_ada,
        g_qkv[...],
        g_attn[...],
        g_in[...],
        g_out[...],
    )
    weights = (
        own_vec[0:9, 0:narrow],
        w_ada[...],
        w_qkv[...],
        w_attn[...],
        w_in[...],
        w_out[...],
    )
    for k in range(6):
        results = adam_step(
            weights[k],
            grads[k] * clip,
            moments[2 * k][...],
            moments[2 * k + 1][...],
            RATE if k else RATE_VECTORS,
            DECAY if k else 0.0,
        )
        for n in range(3):
            outs[3 + 3 * k + n][...] = results[n]


def run_finish(partial_results, weights, moments):
    shapes = [((1, ROWS, WIDTH), BF), ((1, ROWS, WIDTH), F32), ((1, 1), F32)]
    for moment in moments[::2]:
        shapes += [(moment.shape, F32)] * 3
    whole = pl.BlockSpec(memory_space=pltpu.VMEM)
    specs = [whole] * len(shapes)
    specs[2] = pl.BlockSpec(memory_space=pltpu.SMEM)
    args = (*partial_results, *weights, *moments)
    return pl.pallas_call(
        finish_kernel,
        out_shape=[jax.ShapeDtypeStruct(shape, kind) for shape, kind in shapes],
        in_specs=[whole] * len(args),
        out_specs=specs,
        compiler_params=pltpu.CompilerParams(vmem_limit_bytes=60 * 1024 * 1024),
    )(*args)


def slices(
    tokens_in,
    cotangent,
    timesteps,
    span_start,
    span_len,
    vectors,
    w_ada,
    w_qkv,
    w_attn,
    w_in,
    w_out,
    m_vec,
    v_vec,
    m_ada,
    v_ada,
    m_qkv,
    v_qkv,
    m_attn,
    v_attn,
    m_in,
    v_in,
    m_out,
    v_out,
):
    partial_results = run_layer(
        timesteps,
        span_start,
        span_len,
        tokens_in,
        cotangent,
        vectors,
        w_ada.T,
        w_qkv,
        w_attn,
        w_in,
        w_out,
    )
    moments = (
        m_vec,
        v_vec,
        m_ada.T,
        v_ada.T,
        m_qkv,
        v_qkv,
        m_attn,
        v_attn,
        m_in,
        v_in,
        m_out,
        v_out,
    )
    results = run_finish(partial_results, (w_ada.T, w_qkv, w_attn, w_in, w_out), moments)
    ada_results = [result.T for result in results[6:9]]
    return (*results[:2], results[2].reshape(()), *results[3:6], *ada_results, *results[9:])


def solution(mesh):
    in_specs = (
        P("dp", "seq", None),
        P("dp", "seq", None),
        P("dp"),
        P("dp"),
        P("dp"),
        P(),
        P(None, ("dp", "seq")),
        P(("dp", "seq"), None),
        P(("dp", "seq"), None),
        P(("dp", "seq"), None),
        P(("dp", "seq"), None),
        P(None, ("dp", "seq")),
        P(None, ("dp", "seq")),
        P(None, ("dp", "seq")),
        P(None, ("dp", "seq")),
        P(("dp", "seq"), None),
        P(("dp", "seq"), None),
        P(("dp", "seq"), None),
        P(("dp", "seq"), None),
        P(("dp", "seq"), None),
        P(("dp", "seq"), None),
        P(("dp", "seq"), None),
        P(("dp", "seq"), None),
    )
    out_specs = (
        P("dp", "seq", None),
        P("dp", "seq", None),
        P(),
        P(None, ("dp", "seq")),
        P(None, ("dp", "seq")),
        P(None, ("dp", "seq")),
        P(None, ("dp", "seq")),
        P(None, ("dp", "seq")),
        P(None, ("dp", "seq")),
        P(("dp", "seq"), None),
        P(("dp", "seq"), None),
        P(("dp", "seq"), None),
        P(("dp", "seq"), None),
        P(("dp", "seq"), None),
        P(("dp", "seq"), None),
        P(("dp", "seq"), None),
        P(("dp", "seq"), None),
        P(("dp", "seq"), None),
        P(("dp", "seq"), None),
        P(("dp", "seq"), None),
        P(("dp", "seq"), None),
    )
    sizes = dict(mesh.shape)
    local = slices if (sizes["dp"], sizes["seq"]) == (4, 8) else plain
    return jax.shard_map(local, mesh=mesh, in_specs=in_specs, out_specs=out_specs, check_vma=False)
```

```python
from functools import partial
import math
from types import SimpleNamespace

import jax
import jax.numpy as jnp
from jax import lax
from jax.experimental import pallas as pl
from jax.experimental.pallas import tpu as pltpu
from jax.sharding import PartitionSpec as P

HD = 64
COND = 128
STEP = 10


BETA_ONE = 0.9
BETA_TWO = 0.999
ADAM_EPS = 1e-08
RATE = 0.1
RATE_VECTORS = 0.3
DECAY = 0.01
CLIP = 1.0
NORM_EPS = 1e-05


def cond_input(timesteps):
    half_cond = COND // 2
    freqs = jnp.exp(jnp.arange(half_cond, dtype=jnp.float32) * (-math.log(10000.0) / half_cond))
    angles = timesteps.astype(jnp.float32)[:, None] * freqs[None, :]
    return jax.nn.silu(jnp.concatenate([jnp.cos(angles), jnp.sin(angles)], axis=1))


def rotary_tables(positions):
    half_head = HD // 2
    inverse = jnp.exp(jnp.arange(half_head, dtype=jnp.float32) * (-math.log(10000.0) / half_head))
    angles = positions.astype(jnp.float32)[:, None] * inverse[None, :]
    return (jnp.cos(angles), jnp.sin(angles))


def rotate(values, cosines, sines):
    half_head = values.shape[-1] // 2
    first = values[..., :half_head]
    second = values[..., half_head:]
    cos_b = cosines[:, None, :]
    sin_b = sines[:, None, :]
    return jnp.concatenate(
        [first * cos_b - second * sin_b, second * cos_b + first * sin_b], axis=-1
    )


def rotate_back(grads, cosines, sines):
    half_head = grads.shape[-1] // 2
    first = grads[..., :half_head]
    second = grads[..., half_head:]
    cos_b = cosines[:, None, :]
    sin_b = sines[:, None, :]
    return jnp.concatenate(
        [first * cos_b + second * sin_b, second * cos_b - first * sin_b], axis=-1
    )


def normalize(values):
    centre = jnp.mean(values, axis=-1, keepdims=True)
    centred = values - centre
    inverse = lax.rsqrt(jnp.mean(centred * centred, axis=-1, keepdims=True) + NORM_EPS)
    return (centred * inverse, inverse)


def norm_back(normed, inverse, grad):
    return inverse * (
        grad
        - jnp.mean(grad, axis=-1, keepdims=True)
        - normed * jnp.mean(grad * normed, axis=-1, keepdims=True)
    )


def split_kv(block, width):
    seqs, block_rows = (block.shape[0], block.shape[1])
    keys = block[..., :width].reshape(seqs, block_rows, width // HD, HD)
    values = block[..., width:].reshape(seqs, block_rows, width // HD, HD)
    return (keys, values)


def attend_piece(carry, piece, queries, width, factor):
    piece_rows = piece.shape[1]
    size = math.gcd(piece_rows, 512)

    def attend_one_block(index, state):
        running, denom, accum = state
        block = lax.dynamic_slice_in_dim(piece, index * size, size, 1)
        keys, values = split_kv(block, width)
        scores = (
            jnp.einsum("sqhd,skhd->shqk", queries, keys, preferred_element_type=jnp.float32)
            * factor
        )
        highest = jnp.maximum(running, jnp.max(scores, axis=-1))
        shrink = jnp.exp(running - highest)
        weights = jnp.exp(scores - highest[..., None])
        denom = denom * shrink + jnp.sum(weights, axis=-1)
        accum = accum * shrink[..., None] + jnp.einsum(
            "shqk,skhd->shqd",
            weights.astype(jnp.bfloat16),
            values,
            preferred_element_type=jnp.float32,
        )
        return (highest, denom, accum)

    return lax.fori_loop(0, piece_rows // size, attend_one_block, carry)


def block_grads(block, queries, grad_out, logsum, delta, width, factor):
    keys, values = split_kv(block, width)
    scores = (
        jnp.einsum("sqhd,skhd->shqk", queries, keys, preferred_element_type=jnp.float32) * factor
    )
    probs = jnp.exp(scores - logsum[..., None])
    dprobs = jnp.einsum("sqhd,skhd->shqk", grad_out, values, preferred_element_type=jnp.float32)
    dscores = (probs * (dprobs - delta[..., None])).astype(jnp.bfloat16)
    return (keys, probs, dscores)


def query_grads(kv_all, queries, grad_out, logsum, delta, width, factor):
    total_rows = kv_all.shape[1]
    size = math.gcd(total_rows, 512)

    def query_one_block(index, accum):
        block = lax.dynamic_slice_in_dim(kv_all, index * size, size, 1)
        keys, probs, dscores = block_grads(block, queries, grad_out, logsum, delta, width, factor)
        return accum + factor * jnp.einsum(
            "shqk,skhd->sqhd", dscores, keys, preferred_element_type=jnp.float32
        )

    return lax.fori_loop(
        0, total_rows // size, query_one_block, jnp.zeros(queries.shape, jnp.float32)
    )


def key_grads(kv_all, queries, grad_out, logsum, delta, width, factor, count):
    size = math.gcd(count, 512)
    seqs = queries.shape[0]

    def key_one_block(index, accum):
        block = lax.dynamic_slice_in_dim(kv_all, index * size, size, 1)
        keys, probs, dscores = block_grads(block, queries, grad_out, logsum, delta, width, factor)
        grad_vals = jnp.einsum(
            "shqk,sqhd->skhd",
            probs.astype(jnp.bfloat16),
            grad_out,
            preferred_element_type=jnp.float32,
        )
        grad_keys = factor * jnp.einsum(
            "shqk,sqhd->skhd", dscores, queries, preferred_element_type=jnp.float32
        )
        joined = jnp.concatenate(
            [grad_keys.reshape(seqs, size, width), grad_vals.reshape(seqs, size, width)], axis=-1
        )
        return lax.dynamic_update_slice_in_dim(
            accum, jnp.transpose(joined, (1, 0, 2)), index * size, 0
        )

    initial = jnp.zeros((count, seqs, 2 * width), jnp.float32)
    return lax.fori_loop(0, count // size, key_one_block, initial)


def adam_step(weight, grad, first, second, rate, decay_rate):
    new_first = BETA_ONE * first + (1.0 - BETA_ONE) * grad
    new_second = BETA_TWO * second + (1.0 - BETA_TWO) * grad * grad
    fixed_first = new_first / (1.0 - BETA_ONE**STEP)
    fixed_second = new_second / (1.0 - BETA_TWO**STEP)
    new_weight = weight - rate * (
        fixed_first / (jnp.sqrt(fixed_second) + ADAM_EPS) + decay_rate * weight
    )
    return (new_first, new_second, new_weight)


def mod_back(grad_hidden, ln_values, normed, scale_part, gain):
    grad_shift = jnp.sum(grad_hidden, axis=1)
    grad_scale = jnp.sum(grad_hidden * ln_values, axis=1)
    grad_ln = grad_hidden * (1.0 + scale_part)
    grad_gain = jnp.sum(grad_ln * normed, axis=(0, 1))
    return (grad_shift, grad_scale, grad_gain, grad_ln * gain)


def plain(
    tokens_in,
    cotangent,
    timesteps,
    span_start,
    span_len,
    vectors,
    w_ada,
    w_qkv,
    w_attn,
    w_in,
    w_out,
    m_vec,
    v_vec,
    m_ada,
    v_ada,
    m_qkv,
    v_qkv,
    m_attn,
    v_attn,
    m_in,
    v_in,
    m_out,
    v_out,
):
    seqs, group, width = tokens_in.shape
    heads = width // HD
    factor = HD ** (-0.5)
    flat_rows = seqs * group
    full_ada, full_qkv, full_attn, full_in, full_out = (
        lax.all_gather(w_ada.astype(jnp.bfloat16), ("dp", "seq"), axis=1, tiled=True),
        lax.all_gather(w_qkv.astype(jnp.bfloat16), ("dp", "seq"), axis=0, tiled=True),
        lax.all_gather(w_attn.astype(jnp.bfloat16), ("dp", "seq"), axis=0, tiled=True),
        lax.all_gather(w_in.astype(jnp.bfloat16), ("dp", "seq"), axis=0, tiled=True),
        lax.all_gather(w_out.astype(jnp.bfloat16), ("dp", "seq"), axis=0, tiled=True),
    )
    positions = lax.axis_index("seq") * group + jnp.arange(group, dtype=jnp.int32)
    masked = (positions[None, :] >= span_start[:, None]) & (
        positions[None, :] < (span_start + span_len)[:, None]
    )
    cond_bf = cond_input(timesteps).astype(jnp.bfloat16)
    modulation = jnp.dot(cond_bf, full_ada, preferred_element_type=jnp.float32) + vectors[
        2:8
    ].reshape(1, 6 * width)
    pieces = [modulation[:, which * width : (which + 1) * width][:, None, :] for which in range(6)]
    shift_one, scale_one, gate_one, shift_two, scale_two, gate_two = pieces
    start_tokens = jnp.where(
        masked[..., None], vectors[8][None, None, :], tokens_in.astype(jnp.float32)
    )
    normed_one, inv_one = normalize(start_tokens)
    ln_one = normed_one * vectors[0]
    hidden_one = (
        (ln_one * (1.0 + scale_one) + shift_one).astype(jnp.bfloat16).reshape(flat_rows, width)
    )
    projected = jnp.dot(hidden_one, full_qkv, preferred_element_type=jnp.float32).reshape(
        seqs, group, 3 * width
    )
    cosines, sines = rotary_tables(positions)
    queries = rotate(projected[..., :width].reshape(seqs, group, heads, HD), cosines, sines).astype(
        jnp.bfloat16
    )
    keys_here = rotate(
        projected[..., width : 2 * width].reshape(seqs, group, heads, HD), cosines, sines
    ).astype(jnp.bfloat16)
    values_here = projected[..., 2 * width :].astype(jnp.bfloat16)
    kv_local = jnp.concatenate([keys_here.reshape(seqs, group, width), values_here], axis=-1)
    initial = (
        jnp.full((seqs, heads, group), -1e30, jnp.float32),
        jnp.zeros((seqs, heads, group), jnp.float32),
        jnp.zeros((seqs, heads, group, HD), jnp.float32),
    )
    running, denom, accum = attend_piece(
        initial, lax.all_gather(kv_local, "seq", axis=1, tiled=True), queries, width, factor
    )
    attn_heads = accum / denom[..., None]
    logsum = running + jnp.log(denom)
    attn_rows = jnp.transpose(attn_heads, (0, 2, 1, 3)).reshape(flat_rows, width)
    attn_bf = attn_rows.astype(jnp.bfloat16)
    branch_one = jnp.dot(attn_bf, full_attn, preferred_element_type=jnp.float32).reshape(
        seqs, group, width
    )
    mid_tokens = start_tokens + gate_one * branch_one
    normed_two, inv_two = normalize(mid_tokens)
    ln_two = normed_two * vectors[1]
    hidden_two = (
        (ln_two * (1.0 + scale_two) + shift_two).astype(jnp.bfloat16).reshape(flat_rows, width)
    )
    pre_act = jnp.dot(hidden_two, full_in, preferred_element_type=jnp.float32)
    activ, gelu_back = jax.vjp(partial(jax.nn.gelu, approximate=True), pre_act)
    activ_bf = activ.astype(jnp.bfloat16)
    branch_two = jnp.dot(activ_bf, full_out, preferred_element_type=jnp.float32).reshape(
        seqs, group, width
    )
    block_out = (mid_tokens + gate_two * branch_two).astype(jnp.bfloat16)
    grad_y = cotangent.astype(jnp.float32)
    grad_gate_two = jnp.sum(grad_y * branch_two, axis=1)
    grad_branch_two = (grad_y * gate_two).astype(jnp.bfloat16).reshape(flat_rows, width)
    grad_w_out = jnp.dot(activ_bf.T, grad_branch_two, preferred_element_type=jnp.float32)
    grad_activ = jnp.dot(grad_branch_two, full_out.T, preferred_element_type=jnp.float32)
    grad_pre = gelu_back(grad_activ)[0].astype(jnp.bfloat16)
    grad_w_in = jnp.dot(hidden_two.T, grad_pre, preferred_element_type=jnp.float32)
    grad_hidden_two = jnp.dot(grad_pre, full_in.T, preferred_element_type=jnp.float32).reshape(
        seqs, group, width
    )
    grad_shift_two, grad_scale_two, grad_gain_two, grad_normed_two = mod_back(
        grad_hidden_two, ln_two, normed_two, scale_two, vectors[1]
    )
    grad_mid = grad_y + norm_back(normed_two, inv_two, grad_normed_two)
    grad_gate_one = jnp.sum(grad_mid * branch_one, axis=1)
    grad_branch_one = (grad_mid * gate_one).astype(jnp.bfloat16).reshape(flat_rows, width)
    grad_w_attn = jnp.dot(attn_bf.T, grad_branch_one, preferred_element_type=jnp.float32)
    grad_attn_bf = (
        jnp.dot(grad_branch_one, full_attn.T, preferred_element_type=jnp.float32)
        .astype(jnp.bfloat16)
        .reshape(seqs, group, heads, HD)
    )
    delta = jnp.einsum("sqhd,shqd->shq", grad_attn_bf.astype(jnp.float32), attn_heads)
    kv_all = lax.all_gather(kv_local, "seq", axis=1, tiled=True)
    grad_queries = query_grads(kv_all, queries, grad_attn_bf, logsum, delta, width, factor)
    grad_kv = jnp.transpose(
        lax.psum_scatter(
            key_grads(
                kv_all,
                queries,
                grad_attn_bf,
                logsum,
                delta,
                width,
                factor,
                group * lax.axis_size("seq"),
            ).astype(jnp.bfloat16),
            "seq",
            scatter_dimension=0,
            tiled=True,
        ).astype(jnp.float32),
        (1, 0, 2),
    )
    grad_keys = grad_kv[..., :width].reshape(seqs, group, heads, HD)
    grad_qkv = jnp.concatenate(
        [
            rotate_back(grad_queries, cosines, sines).reshape(seqs, group, width),
            rotate_back(grad_keys, cosines, sines).reshape(seqs, group, width),
            grad_kv[..., width:],
        ],
        axis=-1,
    )
    grad_qkv = grad_qkv.astype(jnp.bfloat16).reshape(flat_rows, 3 * width)
    grad_w_qkv = jnp.dot(hidden_one.T, grad_qkv, preferred_element_type=jnp.float32)
    grad_hidden_one = jnp.dot(grad_qkv, full_qkv.T, preferred_element_type=jnp.float32).reshape(
        seqs, group, width
    )
    grad_shift_one, grad_scale_one, grad_gain_one, grad_normed_one = mod_back(
        grad_hidden_one, ln_one, normed_one, scale_one, vectors[0]
    )
    grad_start = grad_mid + norm_back(normed_one, inv_one, grad_normed_one)
    grad_mask_row = jnp.sum(jnp.where(masked[..., None], grad_start, 0.0), axis=(0, 1))
    grad_input = jnp.where(masked[..., None], 0.0, grad_start)
    grad_mod = jnp.concatenate(
        [
            grad_shift_one,
            grad_scale_one,
            grad_gate_one,
            grad_shift_two,
            grad_scale_two,
            grad_gate_two,
        ],
        axis=1,
    )
    grad_w_ada = jnp.dot(cond_bf.astype(jnp.float32).T, grad_mod, precision=lax.Precision.HIGHEST)
    grad_vectors = jnp.concatenate(
        [
            grad_gain_one[None, :],
            grad_gain_two[None, :],
            jnp.sum(grad_mod, axis=0).reshape(6, width),
            grad_mask_row[None, :],
        ],
        axis=0,
    )
    red_ada, red_qkv, red_attn, red_in, red_out, red_vec = (
        lax.psum_scatter(grad_w_ada, ("dp", "seq"), scatter_dimension=1, tiled=True),
        lax.psum_scatter(grad_w_qkv, ("dp", "seq"), scatter_dimension=0, tiled=True),
        lax.psum_scatter(grad_w_attn, ("dp", "seq"), scatter_dimension=0, tiled=True),
        lax.psum_scatter(grad_w_in, ("dp", "seq"), scatter_dimension=0, tiled=True),
        lax.psum_scatter(grad_w_out, ("dp", "seq"), scatter_dimension=0, tiled=True),
        lax.psum_scatter(grad_vectors, ("dp", "seq"), scatter_dimension=1, tiled=True),
    )
    local_squares = jnp.float32(0.0)
    for reduced in (red_vec, red_ada, red_qkv, red_attn, red_in, red_out):
        local_squares = local_squares + jnp.sum(reduced * reduced)
    grad_norm = jnp.sqrt(lax.psum(local_squares, ("dp", "seq")))
    clip_factor = jnp.minimum(1.0, CLIP / (grad_norm + 1e-06))
    columns = red_vec.shape[1]
    own_vectors = lax.dynamic_slice_in_dim(
        vectors, lax.axis_index(("dp", "seq")) * columns, columns, 1
    )
    vec_out = adam_step(own_vectors, red_vec * clip_factor, m_vec, v_vec, RATE_VECTORS, 0.0)
    ada_out = adam_step(w_ada, red_ada * clip_factor, m_ada, v_ada, RATE, DECAY)
    qkv_out = adam_step(w_qkv, red_qkv * clip_factor, m_qkv, v_qkv, RATE, DECAY)
    attn_out = adam_step(w_attn, red_attn * clip_factor, m_attn, v_attn, RATE, DECAY)
    in_out = adam_step(w_in, red_in * clip_factor, m_in, v_in, RATE, DECAY)
    out_out = adam_step(w_out, red_out * clip_factor, m_out, v_out, RATE, DECAY)
    return (
        block_out,
        grad_input,
        grad_norm,
        vec_out[0],
        vec_out[1],
        vec_out[2],
        ada_out[0],
        ada_out[1],
        ada_out[2],
        qkv_out[0],
        qkv_out[1],
        qkv_out[2],
        attn_out[0],
        attn_out[1],
        attn_out[2],
        in_out[0],
        in_out[1],
        in_out[2],
        out_out[0],
        out_out[1],
        out_out[2],
    )


F32, BF = jnp.float32, jnp.bfloat16
MESH = pl.DeviceIdType.MESH
DP, LINE, SEQ, CHIPS, ALL = 4, 4, 8, 16, 32
ROWS, WIDTH, PACK = 128, 768, 640
HALF = WIDTH // 2
HALVES = ((0, 0), (0, 1), (0, 2), (2, 2), (1, 0), (1, 1), (1, 2), None, (2, 0), (2, 1))

def numbered(**counts):
    at = {}
    for name, count in counts.items():
        at[name] = sum(counts[other] for other in at)
    return SimpleNamespace(**at), sum(counts.values())


S, SEM_COUNT = numbered(
    load=11,
    cond=1,
    mix_qkv=1,
    mix_in=1,
    mix_attn=1,
    mod=1,
    w_qkv=1,
    w_attn=4,
    plane_in=1,
    w_in=4,
    w_out=4,
    group_qkv=4,
    group_attn=4,
    fw_qkv=1,
    fw_attn=1,
    fw_in=1,
    fw_out=1,
    tok=4,
    h2=4,
    dm=4,
    xf=4,
    o=1,
    mm=1,
    dh2=1,
    do=1,
    gp=1,
    dh1=5,
    pair_out=1,
    pair_in=1,
    pair_attn=1,
    pair_qkv=1,
    plane_attn=1,
    plane_qkv=1,
    line_out=5,
    line_in=5,
    slice_in=1,
    line_attn=1,
    line_qkv=1,
    last_in=1,
    last_attn=1,
    last_qkv=1,
    early=7,
    late=7,
    sq=1,
)

SCRATCH = dict(
    i_tok=((1, 128, 768), BF),
    i_cot=((1, 128, 768), BF),
    i_vec=((9, 768), F32),
    i_wada=((144, 128), F32),
    i_wqkv=((24, 2304), F32),
    i_wattn=((24, 768), F32),
    i_win=((24, 3072), F32),
    i_wout=((96, 768), F32),
    wide_qkv=((48, 3072), F32),
    wide_in=((48, 3072), F32),
    wide_attn=((48, 768), F32),
    s_qkv=((48, 3072), BF),
    s_in=((48, 3072), BF),
    s_attn=((48, 768), BF),
    w_qkv=((768, 768), BF),
    w_in=((4, 4, 48, 768), BF),
    w_attn=((768, 768), BF),
    w_out=((4, 2, 96, 768), BF),
    t_w_qkv=((640, 768), BF),
    t_w_attn=((768, 1024), BF),
    t_w_in=((768, 768), BF),
    t_w_out=((768, 768), BF),
    t_h1=((768, 512), BF),
    conds_all=((4, 8, 128), F32),
    mod_send=((4, 4, 128), F32),
    mod_got=((32, 4, 128), F32),
    mod_flat=((40, 128), F32),
    mod_pad=((8, 384), F32),
    turn=((2, 4, 128, 128), F32),
    dmod_flat=((4, 40, 128), F32),
    mod=((8, 768), F32),
    x0=((128, 768), F32),
    n1=((4, 128, 768), F32),
    inv1=((4, 128, 128), F32),
    x1=((128, 768), F32),
    n2=((128, 768), F32),
    inv2=((128, 128), F32),
    a=((128, 768), F32),
    dx1=((128, 768), F32),
    toks=((4, 128, 768), BF),
    h1=((4, 128, 768), BF),
    h2=((4, 128, 768), BF),
    dm=((4, 128, 768), BF),
    gb=((4, 128, 768), BF),
    du=((4, 128, 768), BF),
    xb=((2, 4, 128, 640), BF),
    pt=((3, 1024, 512), BF),
    vt=((2, 128, 1024), BF),
    kt=((2, 128, 1024), BF),
    back=((4, 128, 768), F32),
    ot=((2, 128, 512), F32),
    os=((4, 192, 128), BF),
    ob=((4, 192, 128), BF),
    o2=((4, 128, 128), BF),
    mms=((4, 128, 768), BF),
    mmr=((4, 128, 768), BF),
    dhs=((4, 128, 768), BF),
    dhr=((4, 128, 768), BF),
    das=((128, 768), BF),
    dos=((4, 192, 128), BF),
    dob=((4, 192, 128), BF),
    dst=((3, 1024, 512), BF),
    ga=((512, 640), F32),
    gps=((512, 512), BF),
    gpr=((512, 512), BF),
    dqkv=((4, 128, 768), BF),
    d1s=((4, 128, 768), BF),
    d1r=((4, 128, 768), BF),
    g_out=((4, 2, 96, 768), BF),
    g_in=((2, 4, 4, 48, 384), BF),
    g_attn=((2, 768, 384), BF),
    g_qkv=((2, 768, 384), BF),
    p_out=((4, 96, 768), BF),
    p_in=((4, 4, 48, 384), BF),
    p_attn=((768, 384), BF),
    p_qkv=((768, 384), BF),
    q_attn=((4, 192, 384), BF),
    q_qkv=((4, 192, 384), BF),
    m_attn=((192, 384), BF),
    m_qkv=((192, 384), BF),
    r_out=((4, 96, 768), BF),
    r_in=((4, 4, 48, 384), BF),
    via_in=((4, 48, 384), BF),
    via_out=((96, 768), BF),
    via_dh1=((128, 768), BF),
    m_in=((4, 48, 384), BF),
    u_in=((4, 48, 384), BF),
    r_attn=((4, 48, 384), BF),
    r_qkv=((4, 48, 384), BF),
    t_in=((4, 48, 384), F32),
    t_attn=((1, 48, 384), F32),
    t_qkv=((4, 48, 384), F32),
    f_in=((4, 2, 24, 384), F32),
    f_attn=((1, 2, 24, 384), F32),
    f_qkv=((4, 2, 24, 384), F32),
    early=((8, 768), F32),
    early_pair=((8, 768), F32),
    early_line=((4, 8, 384), F32),
    early_plane=((4, 8, 384), F32),
    early_all=((2, 4, 8, 384), F32),
    late=((4, 768), F32),
    late_pair=((4, 768), F32),
    late_line=((4, 4, 384), F32),
    late_plane=((4, 4, 384), F32),
    late_all=((2, 4, 4, 384), F32),
    sq=((32, 1, 128), F32),
)


def dot(left, right):
    return jnp.dot(left, right, preferred_element_type=F32)


def dot_nt(left, right):
    return lax.dot_general(left, right, (((1,), (1,)), ((), ())), preferred_element_type=F32)


def dot_tn(left, right):
    return lax.dot_general(left, right, (((0,), (0,)), ((), ())), preferred_element_type=F32)


def loop(count, body, start=0):
    def step(index, carry):
        body(index)
        return carry

    lax.fori_loop(start, count, step, 0)


def layer_kernel(
    i_time,
    i_start,
    i_len,
    h_tok,
    h_cot,
    h_vec,
    h_wada,
    h_wqkv,
    h_wattn,
    h_win,
    h_wout,
    o_y,
    o_dx,
    o_norm,
    o_gqkv,
    o_gattn,
    o_gin,
    o_gout,
    o_dmod,
    o_gvec,
    o_vec,
    o_conds,
    *scratch,
):
    r = SimpleNamespace(**dict(zip(SCRATCH, scratch)), when=scratch[-3])
    send_sems, recv_sems = scratch[-2:]
    i_tok, i_cot, i_vec, i_wada = r.i_tok, r.i_cot, r.i_vec, r.i_wada
    i_wqkv, i_wattn, i_win, i_wout = r.i_wqkv, r.i_wattn, r.i_win, r.i_wout
    b, s = lax.axis_index("dp"), lax.axis_index("seq")
    z, c = lax.div(s, 2), lax.rem(s, 2)
    mate = s + 1 - 2 * c
    chip = b * LINE + z
    me = b * SEQ + s
    drains = []

    def push(src, dst, at, to_b, to_s, out=None):
        pltpu.make_async_remote_copy(
            src_ref=src,
            dst_ref=dst,
            send_sem=send_sems.at[at if out is None else out],
            recv_sem=recv_sems.at[at],
            device_id=(to_b, to_s),
            device_id_type=MESH,
        ).start()

    def keep(src, dst, at):
        pltpu.make_async_copy(src, dst, recv_sems.at[at]).start()

    def got(at, like):
        pltpu.make_async_copy(like, like, recv_sems.at[at]).wait()

    def left(at, like):
        pltpu.make_async_copy(like, like, send_sems.at[at]).wait()

    def sent(at, like):
        drains.append((at, like))

    near = (b, b + 1 - 2 * lax.rem(b, 2), b + 2 - 4 * lax.div(b, 2), 3 - b)

    def toward(k):
        if k == 3:
            return 3, near[3]
        slot = 1 + c if k == 1 else 2 - c
        return slot, (1 - c) * near[k] + c * near[3 - k]

    def peers(body):
        for k in (1, 2, 3):
            body(*toward(k))

    def stack(body):
        for k in (1, 2, 3):
            body(lax.rem(z + k + 2 * c * (2 - k), LINE))

    def line_gather(block, at, near=True, rest=True):
        inner = 1 + lax.rem(z, 2)
        if near:
            push(block(z), block(z), at + z, b, 2 * inner + c, at)

        def one(to):
            relayed = ((z == 1) & (to == 3)) | ((z == 2) & (to == 0))

            @pl.when(jnp.logical_not(relayed | (to == inner)))
            def _():
                push(block(z), block(z), at + z, b, 2 * to + c, at)

        if rest:
            stack(one)

    def line_relay(block, at):
        for middle, source, to in ((2, 1, 3), (1, 2, 0)):

            @pl.when(z == middle)
            def _():
                got(at + source, block(source))
                push(block(source), block(source), at + source, b, 2 * to + c, at)

    def line_got(block, at, k):
        here = (k == z) | ((z == 2) & (k == 1)) | ((z == 1) & (k == 2))

        @pl.when(jnp.logical_not(here))
        def _():
            got(at + k, block(0))

    far = lax.div(z, 2)

    def line_order(j):
        return lax.rem(z + (2, 3 - 2 * far, 1 + 2 * far, 0)[j], LINE)

    def line_add(j, rows, dst, via, at):
        to = line_order(j)
        outer_chip = (z == 0) | (z == 3)

        def direct():
            push(rows(to), dst.at[z], at + z, b, 2 * to + c, at)

        if j == 0:

            @pl.when(outer_chip)
            def _():
                push(rows(to), via, at + 4, b, 2 * (1 + far) + c, at)

            @pl.when(jnp.logical_not(outer_chip))
            def _():
                direct()

        elif j < 3:
            direct()
        else:
            keep(rows(z), dst.at[z], at + z)

    def line_via(via, at, add):
        @pl.when((z == 1) | (z == 2))
        def _():
            got(at + 4, via)
            add()

    def line_done(dst, at):
        for k in range(4):
            missing = ((z == 1) & (k == 3)) | ((z == 2) & (k == 0))

            @pl.when(jnp.logical_not(missing))
            def _():
                got(at + k, dst.at[k])

    def line_clear(dst):
        for middle, k in ((1, 3), (2, 0)):

            @pl.when(z == middle)
            def _():
                dst[k] = jnp.zeros(dst.shape[1:], BF)

    lane = lax.broadcasted_iota(jnp.int32, (1, 128), 1)
    low = lane < 64
    own24 = pl.ds(pl.multiple_of(24 * c, 8), 24)
    mate24 = pl.ds(pl.multiple_of(24 * (1 - c), 8), 24)
    part = pl.ds(pl.multiple_of(HALF * c, 128), HALF)
    chip_rows = pl.ds(pl.multiple_of(48 * chip, 16), 48)
    group_rows = pl.ds(pl.multiple_of(192 * b, 16), 192)

    barrier = pltpu.get_barrier_semaphore()

    def greet(k):
        other = lax.rem(me + k, ALL)
        pl.semaphore_signal(
            barrier, inc=1, device_id=(lax.div(other, SEQ), lax.rem(other, SEQ)), device_id_type=MESH
        )

    loads = (
        (i_time, r.when.at[0]),
        (i_start, r.when.at[1]),
        (i_len, r.when.at[2]),
        (h_wqkv, i_wqkv),
        (h_win, i_win),
        (h_wattn, i_wattn),
        (h_wout, i_wout),
        (h_tok, i_tok),
        (h_vec, i_vec),
        (h_wada, i_wada),
        (h_cot, i_cot),
    )
    for k, (src, dst) in enumerate(loads):
        pltpu.make_async_copy(src, dst, recv_sems.at[S.load + k]).start()
    loop(ALL, greet, 1)
    for k, (src, dst) in enumerate(loads):
        pltpu.make_async_copy(src, dst, recv_sems.at[S.load + k]).wait()

    def natural(kind, p, head):
        return kind * WIDTH + 192 * p + 64 * head

    def half_at(ref, column, high):
        tile = ref[:, column // 128 * 128 : column // 128 * 128 + 128]
        return tile if (column % 128 == 64) == high else pltpu.roll(tile, 64, 1)

    for p in range(4):
        for tile in range(5):
            pair = []
            for high in (0, 1):
                which = HALVES[2 * tile + high]
                pair.append(
                    jnp.zeros((24, 128), F32)
                    if which is None
                    else half_at(i_wqkv, natural(which[0], p, which[1]), bool(high))
                )
            r.wide_qkv[own24, 768 * p + 128 * tile : 768 * p + 128 * tile + 128] = jnp.where(
                low, pair[0], pair[1]
            )
        r.wide_qkv[own24, 768 * p + 640 : 768 * p + 768] = jnp.zeros((24, 128), F32)
    r.wide_in[own24, :] = i_win[...]
    r.wide_attn[own24, :] = i_wattn[...]
    r.w_out[z, c] = i_wout[...].astype(BF)
    r.toks[z] = i_tok[0]
    line_clear(r.r_out)
    line_clear(r.r_in)
    line_clear(r.d1r)
    lanes8 = lax.broadcasted_iota(jnp.int32, (8, 128), 1)
    half_cond = COND // 2
    speed = jnp.exp((lanes8 % half_cond).astype(F32) * (-math.log(10000.0) / half_cond))
    angle = r.when[0, 0].astype(F32) * speed
    wave = jnp.where(lanes8 < half_cond, jnp.cos(angle), jnp.sin(angle))
    r.conds_all[b] = wave * (1.0 / (1.0 + jnp.exp(-wave)))
    pl.semaphore_wait(barrier, ALL - 1)

    def token_block(k):
        return r.toks.at[k]

    def attn_block(k):
        return r.w_attn.at[pl.ds(pl.multiple_of(192 * b + 48 * k, 16), 48), part]

    def in_block(k):
        return r.w_in.at[:, k, :, part]

    def out_block(k):
        return r.w_out.at[k, c]

    peers(lambda k, to: push(r.conds_all.at[b], r.conds_all.at[b], S.cond, to, s))
    sent(S.cond, r.conds_all.at[0:3])
    push(r.wide_qkv.at[own24], r.wide_qkv.at[own24], S.mix_qkv, b, mate)
    sent(S.mix_qkv, r.wide_qkv.at[0:24])
    push(r.wide_attn.at[own24], r.wide_attn.at[own24], S.mix_attn, b, mate)
    sent(S.mix_attn, r.wide_attn.at[0:24])
    push(r.wide_in.at[own24], r.wide_in.at[own24], S.mix_in, b, mate)
    sent(S.mix_in, r.wide_in.at[0:24])

    got(S.cond, r.conds_all.at[0:3])
    row8 = lax.broadcasted_iota(jnp.int32, (8, 128), 0)
    cond4 = jnp.zeros((8, 128), F32)
    for k in range(4):
        cond4 = jnp.where(row8 == k, r.conds_all[k], cond4)
    o_conds[...] = cond4
    wide = i_wada.shape[0]
    r.mod_pad[...] = jnp.zeros((8, 384), F32)
    r.mod_pad[:, 0:wide] = dot_nt(cond4.astype(BF), i_wada[...].astype(BF))
    columns = pltpu.roll(r.mod_pad[...], lax.rem(wide * me, 128), 1)
    for k in range(4):
        for t in range(3):
            r.mod_send[k, t : t + 1, :] = columns[k : k + 1, 128 * t : 128 * t + 128]
        r.mod_send[k, 3:4, :] = jnp.zeros((1, 128), F32)

    def send_mod(k):
        other = lax.rem(me + k, ALL)
        ob = lax.div(other, SEQ)
        push(r.mod_send.at[ob], r.mod_got.at[me], S.mod, ob, lax.rem(other, SEQ))

    loop(ALL, send_mod, 1)
    sent(S.mod, r.mod_got.at[0:31])
    keep(r.mod_send.at[b], r.mod_got.at[me], S.mod)

    def block(src, first):
        return src.at[:, pl.ds(pl.multiple_of(first, 128), HALF)]

    def along_line(src, dst, at, step):
        stack(
            lambda to: push(
                block(src, step * to + HALF * c), dst.at[chip_rows, part], at, b, 2 * to + c
            )
        )
        keep(block(src, step * z + HALF * c), dst.at[chip_rows, part], at)
        sent(at, dst.at[0:144, 0:HALF])

    def over_plane(dst, at):
        rows = dst.at[group_rows, part]
        peers(lambda k, to: push(rows, rows, at + k, to, s))
        for k in (1, 2, 3):
            sent(at + k, dst.at[0:192, 0:HALF])

    def share(dst, at, onward):
        for k in range(4):
            rows = dst.at[pl.ds(pl.multiple_of(192 * near[k], 16), 192), part]
            if k:
                got(at + k, rows)
            push(rows, rows, onward, b, mate)
        sent(onward, dst.at[:, 0:HALF])

    def line_share(block, at, onward):
        for k in range(4):
            line_got(block, at, k)
            push(block(k), block(k), onward, b, mate)

    got(S.mix_qkv, r.wide_qkv.at[0:24])
    r.s_qkv[...] = r.wide_qkv[...].astype(BF)
    along_line(r.s_qkv, r.w_qkv, S.w_qkv, WIDTH)
    line_gather(token_block, S.tok, rest=False)
    sent(S.tok, r.toks.at[0:3])
    got(S.mix_attn, r.wide_attn.at[0:24])
    r.s_attn[...] = r.wide_attn[...].astype(BF)
    got(S.w_qkv, r.w_qkv.at[0:192, 0:HALF])
    over_plane(r.w_qkv, S.group_qkv)
    line_gather(token_block, S.tok, near=False)
    for h in range(2):

        @pl.when(c == h)
        def _():
            r.w_attn[chip_rows, 384 * h : 384 * h + 384] = r.s_attn[:, 384 * h : 384 * h + 384]

    line_gather(attn_block, S.w_attn)
    sent(S.w_attn, r.w_attn.at[0:144, 0:HALF])
    line_gather(out_block, S.w_out)
    sent(S.w_out, r.w_out.at[0:3, 0])
    got(S.mix_in, r.wide_in.at[0:24])
    r.s_in[...] = r.wide_in[...].astype(BF)
    peers(
        lambda k, to: push(
            block(r.s_in, WIDTH * to + HALF * c), r.w_in.at[b, z, :, part], S.plane_in, to, s
        )
    )
    keep(block(r.s_in, WIDTH * b + HALF * c), r.w_in.at[b, z, :, part], S.plane_in)
    sent(S.plane_in, r.w_in.at[0:3, 0, :, 0:HALF])

    def hidden_rows(k):
        place = (2 * k + c) * ROWS + lax.broadcasted_iota(jnp.int32, (ROWS, 1), 0)
        return (place >= r.when[1, 0]) & (place < r.when[1, 0] + r.when[2, 0])

    def first_norm(tokens, k):
        x0 = jnp.where(hidden_rows(k), i_vec[8:9, :], tokens.astype(F32))
        normed, inverse = normalize(x0)
        r.n1[k] = normed
        r.inv1[k] = jnp.broadcast_to(inverse, (ROWS, 128))
        return x0

    r.x0[...] = first_norm(i_tok[0], z)

    got(S.mod, r.mod_got)
    r.mod_flat[...] = jnp.zeros((40, 128), F32)
    for k in range(ALL):
        first = 9 * k // 8
        r.mod_flat[first : first + 3, :] += r.mod_got[k, 0:3, :]
    for k in range(6):
        row = jnp.concatenate(
            [r.mod_flat[6 * k + t : 6 * k + t + 1, :] for t in range(6)], axis=1
        )
        r.mod[k : k + 1, :] = row + i_vec[2 + k : 3 + k, :]

    def mod(k):
        return r.mod[k : k + 1, :]

    def vec(k):
        return i_vec[k : k + 1, :]

    r.h1[z] = (r.n1[z] * vec(0) * (1.0 + mod(1)) + mod(0)).astype(BF)
    r.dm[0] = (i_cot[0].astype(F32) * mod(5)).astype(BF)
    peers(lambda k, to: push(r.dm.at[0], r.dm.at[k], S.dm + k, to, s))
    for k in (1, 2, 3):
        sent(S.dm + k, r.dm.at[0])

    lanes = lax.broadcasted_iota(jnp.int32, (ROWS, 128), 1)
    first_half = lanes % HD < HD // 2
    speed = jnp.exp((lanes % (HD // 2)).astype(F32) * (-math.log(10000.0) / (HD // 2)))
    row = lax.broadcasted_iota(jnp.int32, (ROWS, 128), 0)

    def table(k):
        angle = ((2 * k + c) * ROWS + row).astype(F32) * speed
        r.turn[0, k] = jnp.cos(angle)
        sine = jnp.sin(angle)
        r.turn[1, k] = jnp.where(first_half, -sine, sine)

    loop(LINE, table)

    line_relay(token_block, S.tok)

    share(r.w_qkv, S.group_qkv, S.fw_qkv)
    got(S.fw_qkv, r.w_qkv.at[:, 0:HALF])
    for k in range(5):
        columns = slice(128 * k, 128 * k + 128)
        r.t_w_qkv[columns, :] = r.w_qkv[:, columns].T

    def turned(tile, sign, k):
        other = jnp.where(first_half, pltpu.roll(tile, 96, 1), pltpu.roll(tile, 32, 1))
        return tile * r.turn[0, k] + sign * (other * r.turn[1, k])

    def project(j):
        k = lax.rem(z + j, LINE)

        @pl.when(j > 0)
        def _():
            line_got(token_block, S.tok, k)
            first_norm(r.toks[k], k)
            r.h1[k] = (r.n1[k] * vec(0) * (1.0 + mod(1)) + mod(0)).astype(BF)

        x = dot(r.h1[k], r.w_qkv[:, 0:PACK])
        tiles = [x[:, 128 * t : 128 * t + 128] for t in range(5)]
        tiles[0] = turned(tiles[0], 1.0, k) * 0.125
        tiles[1] = jnp.where(low, turned(tiles[1], 1.0, k) * 0.125, tiles[1])
        tiles[2] = turned(tiles[2], 1.0, k)
        tiles[3] = turned(tiles[3], 1.0, k)
        for t in range(5):
            r.xb[0, k, :, 128 * t : 128 * t + 128] = tiles[t].astype(BF)
        push(r.xb.at[0, k], r.xb.at[1, k], S.xf + k, b, mate)

    loop(4, project)
    line_relay(attn_block, S.w_attn)
    for k in range(4):
        line_got(attn_block, S.w_attn, k)
    over_plane(r.w_attn, S.group_attn)
    for k in range(4):
        sent(S.xf + k, r.xb.at[0, 0])

    for k in range(4):
        got(S.xf + k, r.xb.at[0, 0])

    def tile_of(t):
        return r.xb[:, :, :, 128 * t : 128 * t + 128].reshape(1024, 128)

    heads = ((0, 2, 4, True, True), (0, 2, 4, False, False), (1, 3, 1, True, False))

    def queries(head, first, size):
        q_tile, _, _, q_low, _ = heads[head]
        q = r.xb[0, first : first + size, :, 128 * q_tile : 128 * q_tile + 128]
        return jnp.where(low if q_low else ~low, q.reshape(size * 128, 128), jnp.zeros((), BF))

    r.vt[0] = tile_of(4).T
    r.vt[1] = tile_of(1).T
    for half in range(2):
        at = slice(256 * half, 256 * half + 256)
        for head in range(3):
            scores = dot_nt(tile_of(heads[head][1]), queries(head, 2 * half, 2))
            weights = jnp.exp(scores - jnp.max(scores, axis=0, keepdims=True))
            weights = weights * (1.0 / jnp.sum(weights, axis=0, keepdims=True))
            weights = weights.astype(BF)
            r.pt[head, :, at] = weights
            out = dot(r.vt[head // 2], weights)
            if head == 0:
                r.ot[0, 0:64, at] = out[0:64]
            elif head == 1:
                r.ot[0, 64:128, at] = out[64:128]
            else:
                r.ot[1, 0:64, at] = out[64:128]
                r.ot[1, 64:128, at] = jnp.zeros((64, 256), F32)
        for k in (2 * half, 2 * half + 1):
            across = slice(128 * k, 128 * k + 128)
            r.os[k, 0:128, :] = r.ot[0, :, across].T.astype(BF)
            third = r.ot[1, 0:64, across]
            third = jnp.concatenate([third, pltpu.roll(third, 64, 1)], axis=0)
            r.os[k, 128:192, :] = third.T[0:64].astype(BF)
        for to in (2 * half, 2 * half + 1):

            @pl.when(z == to)
            def _():
                keep(r.os.at[to], r.ob.at[z], S.o)

            @pl.when(z != to)
            def _():
                push(r.os.at[to], r.ob.at[z], S.o, b, 2 * to + c)

        if half == 0:
            line_relay(out_block, S.w_out)

    sent(S.o, r.os.at[0:3])
    got(S.plane_in, r.w_in.at[:, 0, :, 0:HALF])
    line_gather(in_block, S.w_in)
    sent(S.w_in, r.w_in.at[0:3, :, :, 0:HALF])
    for k in range(2):
        r.kt[k] = tile_of(2 + k).T
    share(r.w_attn, S.group_attn, S.fw_attn)
    got(S.fw_attn, r.w_attn.at[:, 0:HALF])
    for p in range(4):
        first = 192 * p
        r.t_w_attn[:, 256 * p : 256 * p + 128] = r.w_attn[first : first + 128, :].T
        third = r.w_attn[first + 128 : first + 192, :]
        r.t_w_attn[:, 256 * p + 128 : 256 * p + 256] = jnp.concatenate(
            [third, jnp.zeros_like(third)], axis=0
        ).T
    got(S.o, r.ob)
    a = jnp.zeros((ROWS, WIDTH), F32)
    for p in range(4):
        third = r.ob[p, 128:192, :].astype(F32)
        third = jnp.concatenate([third, pltpu.roll(third, 64, 1)], axis=0)
        r.o2[p] = jnp.where(low, third, 0.0).astype(BF)
        a += dot(r.ob[p, 0:128, :], r.w_attn[192 * p : 192 * p + 128, :])
        a += dot(r.o2[p, :, 0:64], r.w_attn[192 * p + 128 : 192 * p + 192, :])
    r.a[...] = a
    x1 = r.x0[...] + mod(2) * a
    r.x1[...] = x1
    n2, inv2 = normalize(x1)
    r.n2[...] = n2
    r.inv2[...] = jnp.broadcast_to(inv2, (ROWS, 128))
    r.h2[0] = (n2 * vec(1) * (1.0 + mod(4)) + mod(3)).astype(BF)
    peers(lambda k, to: push(r.h2.at[0], r.h2.at[k], S.h2 + k, to, s))
    for k in (1, 2, 3):
        sent(S.h2 + k, r.h2.at[0])
    line_relay(in_block, S.w_in)
    line_share(out_block, S.w_out, S.fw_out)
    sent(S.fw_out, r.w_out.at[:, 0])
    got(S.fw_out, r.w_out.at[:, 0])

    for k in range(6):
        columns = slice(128 * k, 128 * k + 128)
        r.t_w_out[columns, :] = r.w_out[:, :, :, columns].reshape(WIDTH, 128).T

    def feed_back(k):
        @pl.when(k > 0)
        def _():
            got(S.dm + k, r.dm.at[0])

        r.back[k] = dot(r.dm[k], r.t_w_out[...])

    loop(4, feed_back)
    line_share(in_block, S.w_in, S.fw_in)
    sent(S.fw_in, r.w_in.at[:, :, :, 0:HALF])
    got(S.fw_in, r.w_in.at[:, :, :, 0:HALF])
    for k in range(6):
        columns = slice(128 * k, 128 * k + 128)
        r.t_w_in[columns, :] = r.w_in[:, :, :, columns].reshape(WIDTH, 128).T

    def feed(first, count):
        at = slice(first, first + count)
        size = count * ROWS
        u = dot(r.h2[at].reshape(size, WIDTH), r.w_in[...].reshape(WIDTH, WIDTH))
        slope = 0.7978845608028654
        cube = 0.044715
        t = jnp.tanh(slope * (u + cube * u * u * u))
        r.gb[at] = (0.5 * u * (1.0 + t)).astype(BF).reshape(count, ROWS, WIDTH)
        bend = 0.5 * (1.0 + t) + 0.5 * u * (1.0 - t * t) * (slope * (1.0 + 3.0 * cube * u * u))
        du = (r.back[at].reshape(size, WIDTH) * bend).astype(BF)
        r.du[at] = du.reshape(count, ROWS, WIDTH)
        r.dhs[at] = dot(du, r.t_w_in[...]).astype(BF).reshape(count, ROWS, WIDTH)

    feed(0, 1)
    for first, count in ((1, 2), (3, 1)):
        for k in range(first, first + count):
            got(S.h2 + k, r.h2.at[0])
        feed(first, count)
        for k in range(first, first + count):
            slot, to = toward(k)
            push(r.dhs.at[slot], r.dhr.at[slot], S.dh2, to, s)
    sent(S.dh2, r.dhs.at[0:3])
    def gather(own, others):
        total = own[0].astype(F32)
        for k in (1, 2, 3):
            total += others[k].astype(F32)
        return total

    for k in range(2):
        rows = slice(384 * k, 384 * k + 384)
        result = dot_tn(r.gb[:, :, rows].reshape(512, 384), r.dm[...].reshape(512, 768))
        r.g_out[2 * k : 2 * k + 2] = result.astype(BF).reshape(2, 2, 96, 768)
    push(r.g_out.at[:, 1 - c], r.p_out, S.pair_out, b, mate)
    sent(S.pair_out, r.p_out)

    def to_mate(grad, dst, at):
        push(grad.at[1 - c], dst, at, b, mate)
        sent(at, dst)

    def pair_sum(grad, pair, at):
        got(at, pair)
        grad[c] = (grad[c].astype(F32) + pair[...].astype(F32)).astype(BF)

    def plane_sum(grad, dst, at):
        def rows(to):
            return grad.at[c, pl.ds(pl.multiple_of(192 * to, 16), 192)]

        peers(lambda k, to: push(rows(to), dst.at[k], at, to, s))
        keep(rows(b), dst.at[0], at)
        sent(at, dst.at[0:3])

    def line_sum(src, total, dst, first, at):
        got(first, src)
        total[...] = (
            (src[0].astype(F32) + src[1].astype(F32)) + (src[2].astype(F32) + src[3].astype(F32))
        ).astype(BF)

        def rows(to):
            return total.at[pl.ds(pl.multiple_of(48 * to, 16), 48)]

        stack(lambda to: push(rows(to), dst.at[z], at, b, 2 * to + c))
        keep(rows(z), dst.at[z], at)
        sent(at, dst.at[0:3])

    def trade(total, final, at):
        push(total.at[:, mate24], final.at[:, c], at, b, mate)
        sent(at, final.at[:, 0])
        final[:, c] = total[:, own24, :]

    def in_product(k):
        rows = slice(384 * k, 384 * k + 384)
        result = dot_tn(r.h2[:, :, rows].reshape(512, 384), r.du[...].reshape(512, 768)).astype(BF)
        for h in range(2):
            r.g_in[h, 2 * k : 2 * k + 2] = result[:, 384 * h : 384 * h + 384].reshape(2, 4, 48, 384)

    in_product(0)

    got(S.pair_out, r.p_out)
    for k in range(4):
        r.g_out[k, c] = (r.g_out[k, c].astype(F32) + r.p_out[k].astype(F32)).astype(BF)

    def out_rows(k):
        return r.g_out.at[k, c]

    for j in (0, 1):
        line_add(j, out_rows, r.r_out, r.via_out, S.line_out)
    in_product(1)
    to_mate(r.g_in, r.p_in, S.pair_in)

    def add_out():
        k = line_order(2)
        r.g_out[k, c] = (r.g_out[k, c].astype(F32) + r.via_out[...].astype(F32)).astype(BF)

    got(S.dh2, r.dhr.at[0:3])
    dh = gather(r.dhs, r.dhr)
    n2 = r.n2[...]
    inv2 = r.inv2[:, 0:1]
    r.early[...] = jnp.zeros((8, 768), F32)
    r.early[2:3, :] = jnp.sum(dh, axis=0, keepdims=True)
    both = jnp.sum(dh * n2, axis=0, keepdims=True)
    r.early[3:4, :] = both * vec(1)
    r.early[0:1, :] = both * (1.0 + mod(4))
    grad = dh * ((1.0 + mod(4)) * vec(1))
    dx1 = i_cot[0].astype(F32) + norm_back(n2, inv2, grad)
    r.dx1[...] = dx1
    r.early[1:2, :] = jnp.sum(dx1 * r.a[...], axis=0, keepdims=True)
    r.das[...] = (dx1 * mod(2)).astype(BF)
    for p in range(4):
        result = dot(r.das[...], r.t_w_attn[:, 256 * p : 256 * p + 256])
        r.dos[p, 0:128, :] = result[:, 0:128].astype(BF)
        third = result[:, 128:256]
        third = jnp.where(low, third[0:64], pltpu.roll(third[64:128], 64, 1))
        r.dos[p, 128:192, :] = third.astype(BF)
    stack(lambda to: push(r.dos.at[to], r.dob.at[z], S.do, b, 2 * to + c))
    keep(r.dos.at[z], r.dob.at[z], S.do)
    sent(S.do, r.dos.at[0:3])
    for t in range(3):
        at = slice(256 * t, 256 * t + 256)
        mm = dot(r.gb[...].reshape(512, WIDTH), r.w_out[:, :, :, at].reshape(WIDTH, 256))
        r.mms[:, :, at] = mm.astype(BF).reshape(4, ROWS, 256)
    peers(lambda k, to: push(r.mms.at[k], r.mmr.at[k], S.mm, to, s))
    sent(S.mm, r.mms.at[0:3])

    for p in range(4):
        for rows, left_side in (
            (slice(192 * p, 192 * p + 128), r.ob[p, 0:128, :]),
            (slice(192 * p + 128, 192 * p + 192), r.o2[p]),
        ):
            result = dot_tn(left_side, r.das[...])[0 : rows.stop - rows.start].astype(BF)
            r.g_attn[0, rows, :] = result[:, 0:HALF]
            r.g_attn[1, rows, :] = result[:, HALF:WIDTH]
    to_mate(r.g_attn, r.p_attn, S.pair_attn)

    def small_sum(src, pair, line, plane, whole, at):
        def first():
            push(src, pair, at, b, mate)
            sent(at, src)

        def second():
            got(at, pair)
            total = src[...] + pair[...]
            line[z] = (1 - c) * total[:, 0:HALF] + c * total[:, HALF:WIDTH]
            stack(lambda to: push(line.at[z], line.at[z], at + 1, b, 2 * to + c))
            sent(at + 1, line.at[0:3])

        def third():
            got(at + 1, line.at[0:3])
            plane[b] = (line[0] + line[1]) + (line[2] + line[3])
            peers(lambda k, to: push(plane.at[b], plane.at[b], at + 2, to, s))
            sent(at + 2, plane.at[0:3])

        def fourth():
            got(at + 2, plane.at[0:3])
            whole[c] = plane[...]
            push(plane, whole.at[c], at + 3, b, mate)
            sent(at + 3, plane)

        def rows(k):
            return jnp.concatenate([whole[0, k], whole[1, k]], axis=1)

        return first, second, third, fourth, rows

    early_steps = small_sum(
        r.early, r.early_pair, r.early_line, r.early_plane, r.early_all, S.early
    )
    late_steps = small_sum(r.late, r.late_pair, r.late_line, r.late_plane, r.late_all, S.late)

    pair_sum(r.g_in, r.p_in, S.pair_in)
    line_via(r.via_out, S.line_out, add_out)
    for j in (2, 3):
        line_add(j, out_rows, r.r_out, r.via_out, S.line_out)
    sent(S.line_out, r.r_out.at[0:3])

    def in_rows(k):
        return r.g_in.at[c, :, k]

    for j in (0, 1):
        line_add(j, in_rows, r.r_in, r.via_in, S.line_in)

    def add_in():
        k = line_order(2)
        r.g_in[c, :, k] = (r.g_in[c, :, k].astype(F32) + r.via_in[...].astype(F32)).astype(BF)

    pair_sum(r.g_attn, r.p_attn, S.pair_attn)
    plane_sum(r.g_attn, r.q_attn, S.plane_attn)

    for k in range(6):
        columns = slice(128 * k, 128 * k + 128)
        r.t_h1[columns, :] = r.h1[:, :, columns].reshape(512, 128).T
    got(S.do, r.dob)
    dot0 = r.dob[:, 0:128, :].reshape(512, 128)
    third = r.dob[:, 128:192, :].astype(F32).reshape(256, 128)
    other_rows = jnp.where(low, pltpu.roll(third, 64, 1), 0.0).reshape(4, 64, 128)
    third = jnp.where(low, third, 0.0).reshape(4, 64, 128)
    dot1 = jnp.concatenate([third, other_rows], axis=1).reshape(512, 128)
    zero = jnp.zeros((), BF)
    moved = pltpu.roll(dot1, 64, 1).astype(BF)
    grads = (jnp.where(low, dot0, zero), jnp.where(low, zero, dot0), moved)
    product = dot0.astype(F32).T * r.ot[0]
    deltas = (
        jnp.sum(product[0:64], axis=0, keepdims=True),
        jnp.sum(product[64:128], axis=0, keepdims=True),
        jnp.sum(dot1.T * r.ot[1], axis=0, keepdims=True),
    )
    for head in range(3):
        values = tile_of(heads[head][2])
        for half in range(2):
            at = slice(256 * half, 256 * half + 256)
            dp = dot_nt(values, grads[head][at])
            r.dst[head, :, at] = (
                r.pt[head, :, at].astype(F32) * (dp - deltas[head][:, at])
            ).astype(BF)

    def key_grads(rows):
        dk = [dot(r.dst[head, rows, :], queries(head, 0, 4)) for head in range(3)]
        dv = [dot(r.pt[head, rows, :], grads[head]) for head in range(3)]
        return (dv[2], dk[0] + dk[1], dk[2], dv[0] + dv[1])

    line_via(r.via_in, S.line_in, add_in)
    for j in (2, 3):
        line_add(j, in_rows, r.r_in, r.via_in, S.line_in)
    sent(S.line_in, r.r_in.at[0:3])
    for t, tile in enumerate(key_grads(slice(512, 1024))):
        r.gps[:, 128 * t : 128 * t + 128] = tile.astype(BF)
    push(r.gps, r.gpr, S.gp, b, mate)
    sent(S.gp, r.gps)
    for t, tile in enumerate(key_grads(slice(0, 512))):
        r.ga[:, 128 * t + 128 : 128 * t + 256] = tile
    for half in range(2):
        at = slice(256 * half, 256 * half + 256)
        turned_q = [dot(r.kt[head // 2], r.dst[head, :, at]) for head in range(3)]
        top = jnp.concatenate([turned_q[0][0:64], turned_q[1][64:128]], axis=0)
        r.ga[at, 0:128] = top.T * 0.125
        r.ga[at, 128:256] += turned_q[2].T * 0.125
    got(S.mm, r.mmr.at[0:3])
    mm = gather(r.mms, r.mmr)
    o_y[...] = (r.x1[...] + mod(5) * mm).astype(BF)
    r.early[4:5, :] = jnp.sum(i_cot[0].astype(F32) * mm, axis=0, keepdims=True)
    early_steps[0]()
    got(S.gp, r.gpr)

    def dh1_rows(k):
        return r.d1s.at[k]

    def back_turn(k):
        rows = pl.ds(pl.multiple_of(128 * k, 128), 128)
        tiles = [r.ga[rows, 0:128]] + [
            r.ga[rows, 128 * t : 128 * t + 128]
            + r.gpr[rows, 128 * t - 128 : 128 * t].astype(F32)
            for t in range(1, 5)
        ]
        tiles[0] = turned(tiles[0], -1.0, k)
        tiles[1] = jnp.where(low, turned(tiles[1], -1.0, k), tiles[1])
        tiles[2] = turned(tiles[2], -1.0, k)
        tiles[3] = turned(tiles[3], -1.0, k)
        for t in range(5):
            r.dqkv[k, :, 128 * t : 128 * t + 128] = tiles[t].astype(BF)
        r.dqkv[k, :, PACK:WIDTH] = jnp.zeros((128, 128), BF)

    loop(4, back_turn)
    early_steps[1]()

    def unproject(j):
        k = line_order(j)
        partial_sum = dot(r.dqkv[k, :, 0:PACK], r.t_w_qkv[...])
        r.d1s[k] = partial_sum.astype(BF)
        if j == 2:

            def add():
                r.d1s[k] = (partial_sum + r.via_dh1[...].astype(F32)).astype(BF)

            line_via(r.via_dh1, S.dh1, add)
        line_add(j, dh1_rows, r.d1r, r.via_dh1, S.dh1)
        n = r.n1[k]
        e = partial_sum * ((1.0 + mod(1)) * vec(0))
        weight = jnp.where(hidden_rows(k), r.inv1[k][:, 0:1], 0.0)
        centred = (
            e
            - jnp.mean(e, axis=-1, keepdims=True)
            - n * jnp.mean(e * n, axis=-1, keepdims=True)
        )
        r.late[0:1, :] += jnp.sum(partial_sum * n, axis=0, keepdims=True)
        r.late[1:2, :] += jnp.sum(partial_sum, axis=0, keepdims=True)
        r.late[3:4, :] += jnp.sum(weight * centred, axis=0, keepdims=True)

    r.late[...] = jnp.zeros((4, 768), F32)
    r.late[3:4, :] = jnp.sum(
        jnp.where(hidden_rows(z), r.dx1[...], 0.0), axis=0, keepdims=True
    )
    unproject(0)

    def qkv_rows(k):
        rows = pl.ds(pl.multiple_of(128 * k, 128), 128)
        result = dot(r.t_h1[rows, :], r.dqkv[...].reshape(512, WIDTH)).astype(BF)
        r.g_qkv[0, rows, :] = result[:, 0:HALF]
        r.g_qkv[1, rows, :] = result[:, HALF:WIDTH]

    loop(6, qkv_rows)
    to_mate(r.g_qkv, r.p_qkv, S.pair_qkv)
    unproject(1)
    pair_sum(r.g_qkv, r.p_qkv, S.pair_qkv)
    plane_sum(r.g_qkv, r.q_qkv, S.plane_qkv)
    early_steps[2]()
    unproject(2)
    unproject(3)
    sent(S.dh1, r.d1s.at[0:3])
    both = r.late[0:1, :]
    r.late[2:3, :] = both * vec(0)
    r.late[0:1, :] = both * (1.0 + mod(1))
    late_steps[0]()
    early_steps[3]()
    line_sum(r.q_attn, r.m_attn, r.r_attn, S.plane_attn, S.line_attn)
    late_steps[1]()

    line_done(r.r_in, S.line_in)
    r.m_in[...] = (
        (r.r_in[0].astype(F32) + r.r_in[1].astype(F32))
        + (r.r_in[2].astype(F32) + r.r_in[3].astype(F32))
    ).astype(BF)
    peers(lambda k, to: push(r.m_in.at[to], r.u_in.at[b], S.slice_in, to, s))
    keep(r.m_in.at[b], r.u_in.at[b], S.slice_in)
    sent(S.slice_in, r.u_in.at[0:3])
    late_steps[2]()
    line_sum(r.q_qkv, r.m_qkv, r.r_qkv, S.plane_qkv, S.line_qkv)

    line_done(r.d1r, S.dh1)
    dh = (r.d1r[0].astype(F32) + r.d1r[1].astype(F32)) + (
        r.d1r[2].astype(F32) + r.d1r[3].astype(F32)
    )
    n1 = r.n1[z]
    grad = dh * ((1.0 + mod(1)) * vec(0))
    dx0 = r.dx1[...] + norm_back(n1, r.inv1[z][:, 0:1], grad)
    o_dx[...] = jnp.where(hidden_rows(z), 0.0, dx0)
    late_steps[3]()

    line_done(r.r_out, S.line_out)
    total = (r.r_out[0].astype(F32) + r.r_out[1].astype(F32)) + (
        r.r_out[2].astype(F32) + r.r_out[3].astype(F32)
    )
    o_gout[...] = total
    squares = total * total
    squares = jnp.sum(squares[:, 0:128] + squares[:, 128:256] + squares[:, 256:384]
                      + squares[:, 384:512] + squares[:, 512:640] + squares[:, 640:768],
                      axis=0, keepdims=True)

    def fold(value):
        total = value[:, 0:128] * value[:, 0:128]
        for t in range(1, value.shape[1] // 128):
            total += value[:, 128 * t : 128 * t + 128] * value[:, 128 * t : 128 * t + 128]
        return jnp.sum(total, axis=0, keepdims=True)

    got(S.slice_in, r.u_in)
    r.t_in[...] = r.u_in[...].astype(F32)
    for p in range(4):
        squares += fold(r.t_in[p])
    trade(r.t_in, r.f_in, S.last_in)
    got(S.line_attn, r.r_attn)
    r.t_attn[0] = (r.r_attn[0].astype(F32) + r.r_attn[1].astype(F32)) + (
        r.r_attn[2].astype(F32) + r.r_attn[3].astype(F32)
    )
    squares += fold(r.t_attn[0])
    trade(r.t_attn, r.f_attn, S.last_attn)
    got(S.line_qkv, r.r_qkv)
    r.t_qkv[...] = r.r_qkv[...].astype(F32)
    trade(r.t_qkv, r.f_qkv, S.last_qkv)
    for p in range(4):
        squares += fold(r.t_qkv[p])
    r.sq[me] = squares

    def send_sq(k):
        other = lax.rem(me + k, ALL)
        push(r.sq.at[me], r.sq.at[me], S.sq, lax.div(other, SEQ), lax.rem(other, SEQ))

    loop(ALL, send_sq, 1)
    sent(S.sq, r.sq.at[0:31])
    got(S.last_in, r.f_in.at[:, 0])
    got(S.last_attn, r.f_attn.at[:, 0])
    for h in range(2):
        for p in range(4):
            value = r.f_in[p, h]
            o_gin[:, 768 * p + 384 * h : 768 * p + 384 * h + 384] = value
        value = r.f_attn[0, h]
        o_gattn[:, 384 * h : 384 * h + 384] = value
    got(S.last_qkv, r.f_qkv.at[:, 0])
    where = {which: index for index, which in enumerate(HALVES) if which is not None}

    def packed_half(chunk, high):
        kind, rest = chunk // 12, chunk % 12
        index = where[(kind, rest % 3)]
        t = index // 2
        tile = r.f_qkv[rest // 3, t // 3, :, t % 3 * 128 : t % 3 * 128 + 128]
        return tile if index % 2 == high else pltpu.roll(tile, 64, 1)

    for t in range(18):
        o_gqkv[:, 128 * t : 128 * t + 128] = jnp.where(
            low, packed_half(2 * t, 0), packed_half(2 * t + 1, 1)
        )
    got(S.early + 3, r.early_all.at[0])
    got(S.late + 3, r.late_all.at[0])
    early_rows = [early_steps[4](k) for k in range(4)]
    late_rows = [late_steps[4](k) for k in range(4)]
    mods = []
    for k in range(4):
        early, late = early_rows[k], late_rows[k]
        rows = jnp.concatenate([late[1:3], early[1:5], jnp.zeros((2, 768), F32)], axis=0)
        for n in range(6):
            for m in range(6):
                r.dmod_flat[k, 6 * n + m : 6 * n + m + 1, :] = rows[
                    n : n + 1, 128 * m : 128 * m + 128
                ]
        mods.append(rows)
    gain = jnp.concatenate(
        [
            sum(late_rows[k][0:1] for k in range(4)),
            sum(early_rows[k][0:1] for k in range(4)),
            (mods[0] + mods[1] + mods[2] + mods[3])[0:6],
        ],
        axis=0,
    )
    mask_row = sum(late_rows[k][3:4] for k in range(4))
    gains = jnp.concatenate([gain, mask_row, jnp.zeros((7, 768), F32)], axis=0)
    masters = jnp.concatenate([i_vec[...], jnp.zeros((7, 768), F32)], axis=0)
    own = lax.rem(WIDTH - 24 * me, WIDTH)
    o_gvec[...] = pltpu.roll(gains, own, 1)[:, 0:128]
    o_vec[...] = pltpu.roll(masters, own, 1)[:, 0:128]
    r.mod_pad[...] = jnp.zeros((8, 384), F32)
    window = lax.div(wide * me, 128)
    for k in range(4):
        rows = r.dmod_flat[k, pl.ds(window, 3), :]
        for m in range(3):
            r.mod_pad[k : k + 1, 128 * m : 128 * m + 128] = rows[m : m + 1, :]
    o_dmod[...] = pltpu.roll(r.mod_pad[...], lax.rem(384 - lax.rem(wide * me, 128), 384), 1)[:, 0:256]
    small = jnp.sum(gain * gain) + jnp.sum(mask_row * mask_row)
    conds = [r.conds_all[k][0:1].astype(BF).astype(F32) for k in range(4)]
    for k in range(4):
        for m in range(k, 4):
            term = jnp.sum(mods[k] * mods[m]) * jnp.sum(conds[k] * conds[m])
            small += term if m == k else 2.0 * term
    got(S.sq, r.sq.at[0:31])
    total = r.sq[0]
    for k in range(1, ALL):
        total += r.sq[k]
    o_norm[...] = jnp.broadcast_to(jnp.sqrt(jnp.sum(total) + small), (8, 128))

    for at, like in drains:
        left(at, like)


def run_layer(*args):
    shapes = (
        ((ROWS, WIDTH), BF),
        ((ROWS, WIDTH), F32),
        ((8, 128), F32),
        ((24, 3 * WIDTH), F32),
        ((24, WIDTH), F32),
        ((24, 4 * WIDTH), F32),
        ((96, WIDTH), F32),
        ((8, 256), F32),
        ((16, 128), F32),
        ((16, 128), F32),
        ((8, 128), F32),
    )
    whole = pl.BlockSpec(memory_space=pltpu.VMEM)
    return pl.pallas_call(
        layer_kernel,
        out_shape=[jax.ShapeDtypeStruct(shape, kind) for shape, kind in shapes],
        in_specs=[pl.BlockSpec(memory_space=pl.ANY)] * len(args),
        out_specs=[whole] * len(shapes),
        scratch_shapes=[pltpu.VMEM(shape, kind) for shape, kind in SCRATCH.values()]
        + [pltpu.SMEM((3, 1), jnp.int32)]
        + [pltpu.SemaphoreType.DMA((SEM_COUNT,)), pltpu.SemaphoreType.DMA((SEM_COUNT,))],
        compiler_params=pltpu.CompilerParams(
            collective_id=0, has_side_effects=True, vmem_limit_bytes=60 * 1024 * 1024
        ),
    )(*args)


def finish_kernel(
    y, dx, norm, g_qkv, g_attn, g_in, g_out, dmod, g_vec, own_vec, conds, *rest
):
    (w_ada, w_qkv, w_attn, w_in, w_out), moments, outs = rest[:5], rest[5:17], rest[17:]
    outs[0][0] = y[...]
    outs[1][0] = dx[...]
    outs[2][0, 0] = norm[0, 0]
    clip = jnp.minimum(1.0, CLIP / (norm[0:1, 0:1] + 1e-06))
    columns = w_ada.shape[0]
    rounded = conds[...].astype(BF).astype(F32)
    turned_mod = dmod[...].T
    g_ada = turned_mod[0:columns, 0:1] * rounded[0:1, :]
    for k in range(1, 4):
        g_ada += turned_mod[0:columns, k : k + 1] * rounded[k : k + 1, :]
    narrow = moments[0].shape[1]
    grads = (
        g_vec[0:9, 0:narrow],
        g_ada,
        g_qkv[...],
        g_attn[...],
        g_in[...],
        g_out[...],
    )
    weights = (
        own_vec[0:9, 0:narrow],
        w_ada[...],
        w_qkv[...],
        w_attn[...],
        w_in[...],
        w_out[...],
    )
    for k in range(6):
        results = adam_step(
            weights[k],
            grads[k] * clip,
            moments[2 * k][...],
            moments[2 * k + 1][...],
            RATE if k else RATE_VECTORS,
            DECAY if k else 0.0,
        )
        for n in range(3):
            outs[3 + 3 * k + n][...] = results[n]


def run_finish(partial_results, weights, moments):
    shapes = [((1, ROWS, WIDTH), BF), ((1, ROWS, WIDTH), F32), ((1, 1), F32)]
    for moment in moments[::2]:
        shapes += [(moment.shape, F32)] * 3
    whole = pl.BlockSpec(memory_space=pltpu.VMEM)
    specs = [whole] * len(shapes)
    specs[2] = pl.BlockSpec(memory_space=pltpu.SMEM)
    args = (*partial_results, *weights, *moments)
    return pl.pallas_call(
        finish_kernel,
        out_shape=[jax.ShapeDtypeStruct(shape, kind) for shape, kind in shapes],
        in_specs=[whole] * len(args),
        out_specs=specs,
        compiler_params=pltpu.CompilerParams(vmem_limit_bytes=60 * 1024 * 1024),
    )(*args)


def slices(
    tokens_in,
    cotangent,
    timesteps,
    span_start,
    span_len,
    vectors,
    w_ada,
    w_qkv,
    w_attn,
    w_in,
    w_out,
    m_vec,
    v_vec,
    m_ada,
    v_ada,
    m_qkv,
    v_qkv,
    m_attn,
    v_attn,
    m_in,
    v_in,
    m_out,
    v_out,
):
    partial_results = run_layer(
        timesteps,
        span_start,
        span_len,
        tokens_in,
        cotangent,
        vectors,
        w_ada.T,
        w_qkv,
        w_attn,
        w_in,
        w_out,
    )
    moments = (
        m_vec,
        v_vec,
        m_ada.T,
        v_ada.T,
        m_qkv,
        v_qkv,
        m_attn,
        v_attn,
        m_in,
        v_in,
        m_out,
        v_out,
    )
    results = run_finish(partial_results, (w_ada.T, w_qkv, w_attn, w_in, w_out), moments)
    ada_results = [result.T for result in results[6:9]]
    return (*results[:2], results[2].reshape(()), *results[3:6], *ada_results, *results[9:])


def solution(mesh):
    in_specs = (
        P("dp", "seq", None),
        P("dp", "seq", None),
        P("dp"),
        P("dp"),
        P("dp"),
        P(),
        P(None, ("dp", "seq")),
        P(("dp", "seq"), None),
        P(("dp", "seq"), None),
        P(("dp", "seq"), None),
        P(("dp", "seq"), None),
        P(None, ("dp", "seq")),
        P(None, ("dp", "seq")),
        P(None, ("dp", "seq")),
        P(None, ("dp", "seq")),
        P(("dp", "seq"), None),
        P(("dp", "seq"), None),
        P(("dp", "seq"), None),
        P(("dp", "seq"), None),
        P(("dp", "seq"), None),
        P(("dp", "seq"), None),
        P(("dp", "seq"), None),
        P(("dp", "seq"), None),
    )
    out_specs = (
        P("dp", "seq", None),
        P("dp", "seq", None),
        P(),
        P(None, ("dp", "seq")),
        P(None, ("dp", "seq")),
        P(None, ("dp", "seq")),
        P(None, ("dp", "seq")),
        P(None, ("dp", "seq")),
        P(None, ("dp", "seq")),
        P(("dp", "seq"), None),
        P(("dp", "seq"), None),
        P(("dp", "seq"), None),
        P(("dp", "seq"), None),
        P(("dp", "seq"), None),
        P(("dp", "seq"), None),
        P(("dp", "seq"), None),
        P(("dp", "seq"), None),
        P(("dp", "seq"), None),
        P(("dp", "seq"), None),
        P(("dp", "seq"), None),
        P(("dp", "seq"), None),
    )
    sizes = dict(mesh.shape)
    local = slices if (sizes["dp"], sizes["seq"]) == (4, 8) else plain
    return jax.shard_map(local, mesh=mesh, in_specs=in_specs, out_specs=out_specs, check_vma=False)
```

```python
from functools import partial
import math
from types import SimpleNamespace

import jax
import jax.numpy as jnp
from jax import lax
from jax.experimental import pallas as pl
from jax.experimental.pallas import tpu as pltpu
from jax.sharding import PartitionSpec as P

HD = 64
COND = 128
STEP = 10


BETA_ONE = 0.9
BETA_TWO = 0.999
ADAM_EPS = 1e-08
RATE = 0.1
RATE_VECTORS = 0.3
DECAY = 0.01
CLIP = 1.0
NORM_EPS = 1e-05


def cond_input(timesteps):
    half_cond = COND // 2
    freqs = jnp.exp(jnp.arange(half_cond, dtype=jnp.float32) * (-math.log(10000.0) / half_cond))
    angles = timesteps.astype(jnp.float32)[:, None] * freqs[None, :]
    return jax.nn.silu(jnp.concatenate([jnp.cos(angles), jnp.sin(angles)], axis=1))


def rotary_tables(positions):
    half_head = HD // 2
    inverse = jnp.exp(jnp.arange(half_head, dtype=jnp.float32) * (-math.log(10000.0) / half_head))
    angles = positions.astype(jnp.float32)[:, None] * inverse[None, :]
    return (jnp.cos(angles), jnp.sin(angles))


def rotate(values, cosines, sines):
    half_head = values.shape[-1] // 2
    first = values[..., :half_head]
    second = values[..., half_head:]
    cos_b = cosines[:, None, :]
    sin_b = sines[:, None, :]
    return jnp.concatenate(
        [first * cos_b - second * sin_b, second * cos_b + first * sin_b], axis=-1
    )


def rotate_back(grads, cosines, sines):
    half_head = grads.shape[-1] // 2
    first = grads[..., :half_head]
    second = grads[..., half_head:]
    cos_b = cosines[:, None, :]
    sin_b = sines[:, None, :]
    return jnp.concatenate(
        [first * cos_b + second * sin_b, second * cos_b - first * sin_b], axis=-1
    )


def normalize(values):
    centre = jnp.mean(values, axis=-1, keepdims=True)
    centred = values - centre
    inverse = lax.rsqrt(jnp.mean(centred * centred, axis=-1, keepdims=True) + NORM_EPS)
    return (centred * inverse, inverse)


def norm_back(normed, inverse, grad):
    return inverse * (
        grad
        - jnp.mean(grad, axis=-1, keepdims=True)
        - normed * jnp.mean(grad * normed, axis=-1, keepdims=True)
    )


def split_kv(block, width):
    seqs, block_rows = (block.shape[0], block.shape[1])
    keys = block[..., :width].reshape(seqs, block_rows, width // HD, HD)
    values = block[..., width:].reshape(seqs, block_rows, width // HD, HD)
    return (keys, values)


def attend_piece(carry, piece, queries, width, factor):
    piece_rows = piece.shape[1]
    size = math.gcd(piece_rows, 512)

    def attend_one_block(index, state):
        running, denom, accum = state
        block = lax.dynamic_slice_in_dim(piece, index * size, size, 1)
        keys, values = split_kv(block, width)
        scores = (
            jnp.einsum("sqhd,skhd->shqk", queries, keys, preferred_element_type=jnp.float32)
            * factor
        )
        highest = jnp.maximum(running, jnp.max(scores, axis=-1))
        shrink = jnp.exp(running - highest)
        weights = jnp.exp(scores - highest[..., None])
        denom = denom * shrink + jnp.sum(weights, axis=-1)
        accum = accum * shrink[..., None] + jnp.einsum(
            "shqk,skhd->shqd",
            weights.astype(jnp.bfloat16),
            values,
            preferred_element_type=jnp.float32,
        )
        return (highest, denom, accum)

    return lax.fori_loop(0, piece_rows // size, attend_one_block, carry)


def block_grads(block, queries, grad_out, logsum, delta, width, factor):
    keys, values = split_kv(block, width)
    scores = (
        jnp.einsum("sqhd,skhd->shqk", queries, keys, preferred_element_type=jnp.float32) * factor
    )
    probs = jnp.exp(scores - logsum[..., None])
    dprobs = jnp.einsum("sqhd,skhd->shqk", grad_out, values, preferred_element_type=jnp.float32)
    dscores = (probs * (dprobs - delta[..., None])).astype(jnp.bfloat16)
    return (keys, probs, dscores)


def query_grads(kv_all, queries, grad_out, logsum, delta, width, factor):
    total_rows = kv_all.shape[1]
    size = math.gcd(total_rows, 512)

    def query_one_block(index, accum):
        block = lax.dynamic_slice_in_dim(kv_all, index * size, size, 1)
        keys, probs, dscores = block_grads(block, queries, grad_out, logsum, delta, width, factor)
        return accum + factor * jnp.einsum(
            "shqk,skhd->sqhd", dscores, keys, preferred_element_type=jnp.float32
        )

    return lax.fori_loop(
        0, total_rows // size, query_one_block, jnp.zeros(queries.shape, jnp.float32)
    )


def key_grads(kv_all, queries, grad_out, logsum, delta, width, factor, count):
    size = math.gcd(count, 512)
    seqs = queries.shape[0]

    def key_one_block(index, accum):
        block = lax.dynamic_slice_in_dim(kv_all, index * size, size, 1)
        keys, probs, dscores = block_grads(block, queries, grad_out, logsum, delta, width, factor)
        grad_vals = jnp.einsum(
            "shqk,sqhd->skhd",
            probs.astype(jnp.bfloat16),
            grad_out,
            preferred_element_type=jnp.float32,
        )
        grad_keys = factor * jnp.einsum(
            "shqk,sqhd->skhd", dscores, queries, preferred_element_type=jnp.float32
        )
        joined = jnp.concatenate(
            [grad_keys.reshape(seqs, size, width), grad_vals.reshape(seqs, size, width)], axis=-1
        )
        return lax.dynamic_update_slice_in_dim(
            accum, jnp.transpose(joined, (1, 0, 2)), index * size, 0
        )

    initial = jnp.zeros((count, seqs, 2 * width), jnp.float32)
    return lax.fori_loop(0, count // size, key_one_block, initial)


def adam_step(weight, grad, first, second, rate, decay_rate):
    new_first = BETA_ONE * first + (1.0 - BETA_ONE) * grad
    new_second = BETA_TWO * second + (1.0 - BETA_TWO) * grad * grad
    fixed_first = new_first / (1.0 - BETA_ONE**STEP)
    fixed_second = new_second / (1.0 - BETA_TWO**STEP)
    new_weight = weight - rate * (
        fixed_first / (jnp.sqrt(fixed_second) + ADAM_EPS) + decay_rate * weight
    )
    return (new_first, new_second, new_weight)


def mod_back(grad_hidden, ln_values, normed, scale_part, gain):
    grad_shift = jnp.sum(grad_hidden, axis=1)
    grad_scale = jnp.sum(grad_hidden * ln_values, axis=1)
    grad_ln = grad_hidden * (1.0 + scale_part)
    grad_gain = jnp.sum(grad_ln * normed, axis=(0, 1))
    return (grad_shift, grad_scale, grad_gain, grad_ln * gain)


def plain(
    tokens_in,
    cotangent,
    timesteps,
    span_start,
    span_len,
    vectors,
    w_ada,
    w_qkv,
    w_attn,
    w_in,
    w_out,
    m_vec,
    v_vec,
    m_ada,
    v_ada,
    m_qkv,
    v_qkv,
    m_attn,
    v_attn,
    m_in,
    v_in,
    m_out,
    v_out,
):
    seqs, group, width = tokens_in.shape
    heads = width // HD
    factor = HD ** (-0.5)
    flat_rows = seqs * group
    full_ada, full_qkv, full_attn, full_in, full_out = (
        lax.all_gather(w_ada.astype(jnp.bfloat16), ("dp", "seq"), axis=1, tiled=True),
        lax.all_gather(w_qkv.astype(jnp.bfloat16), ("dp", "seq"), axis=0, tiled=True),
        lax.all_gather(w_attn.astype(jnp.bfloat16), ("dp", "seq"), axis=0, tiled=True),
        lax.all_gather(w_in.astype(jnp.bfloat16), ("dp", "seq"), axis=0, tiled=True),
        lax.all_gather(w_out.astype(jnp.bfloat16), ("dp", "seq"), axis=0, tiled=True),
    )
    positions = lax.axis_index("seq") * group + jnp.arange(group, dtype=jnp.int32)
    masked = (positions[None, :] >= span_start[:, None]) & (
        positions[None, :] < (span_start + span_len)[:, None]
    )
    cond_bf = cond_input(timesteps).astype(jnp.bfloat16)
    modulation = jnp.dot(cond_bf, full_ada, preferred_element_type=jnp.float32) + vectors[
        2:8
    ].reshape(1, 6 * width)
    pieces = [modulation[:, which * width : (which + 1) * width][:, None, :] for which in range(6)]
    shift_one, scale_one, gate_one, shift_two, scale_two, gate_two = pieces
    start_tokens = jnp.where(
        masked[..., None], vectors[8][None, None, :], tokens_in.astype(jnp.float32)
    )
    normed_one, inv_one = normalize(start_tokens)
    ln_one = normed_one * vectors[0]
    hidden_one = (
        (ln_one * (1.0 + scale_one) + shift_one).astype(jnp.bfloat16).reshape(flat_rows, width)
    )
    projected = jnp.dot(hidden_one, full_qkv, preferred_element_type=jnp.float32).reshape(
        seqs, group, 3 * width
    )
    cosines, sines = rotary_tables(positions)
    queries = rotate(projected[..., :width].reshape(seqs, group, heads, HD), cosines, sines).astype(
        jnp.bfloat16
    )
    keys_here = rotate(
        projected[..., width : 2 * width].reshape(seqs, group, heads, HD), cosines, sines
    ).astype(jnp.bfloat16)
    values_here = projected[..., 2 * width :].astype(jnp.bfloat16)
    kv_local = jnp.concatenate([keys_here.reshape(seqs, group, width), values_here], axis=-1)
    initial = (
        jnp.full((seqs, heads, group), -1e30, jnp.float32),
        jnp.zeros((seqs, heads, group), jnp.float32),
        jnp.zeros((seqs, heads, group, HD), jnp.float32),
    )
    running, denom, accum = attend_piece(
        initial, lax.all_gather(kv_local, "seq", axis=1, tiled=True), queries, width, factor
    )
    attn_heads = accum / denom[..., None]
    logsum = running + jnp.log(denom)
    attn_rows = jnp.transpose(attn_heads, (0, 2, 1, 3)).reshape(flat_rows, width)
    attn_bf = attn_rows.astype(jnp.bfloat16)
    branch_one = jnp.dot(attn_bf, full_attn, preferred_element_type=jnp.float32).reshape(
        seqs, group, width
    )
    mid_tokens = start_tokens + gate_one * branch_one
    normed_two, inv_two = normalize(mid_tokens)
    ln_two = normed_two * vectors[1]
    hidden_two = (
        (ln_two * (1.0 + scale_two) + shift_two).astype(jnp.bfloat16).reshape(flat_rows, width)
    )
    pre_act = jnp.dot(hidden_two, full_in, preferred_element_type=jnp.float32)
    activ, gelu_back = jax.vjp(partial(jax.nn.gelu, approximate=True), pre_act)
    activ_bf = activ.astype(jnp.bfloat16)
    branch_two = jnp.dot(activ_bf, full_out, preferred_element_type=jnp.float32).reshape(
        seqs, group, width
    )
    block_out = (mid_tokens + gate_two * branch_two).astype(jnp.bfloat16)
    grad_y = cotangent.astype(jnp.float32)
    grad_gate_two = jnp.sum(grad_y * branch_two, axis=1)
    grad_branch_two = (grad_y * gate_two).astype(jnp.bfloat16).reshape(flat_rows, width)
    grad_w_out = jnp.dot(activ_bf.T, grad_branch_two, preferred_element_type=jnp.float32)
    grad_activ = jnp.dot(grad_branch_two, full_out.T, preferred_element_type=jnp.float32)
    grad_pre = gelu_back(grad_activ)[0].astype(jnp.bfloat16)
    grad_w_in = jnp.dot(hidden_two.T, grad_pre, preferred_element_type=jnp.float32)
    grad_hidden_two = jnp.dot(grad_pre, full_in.T, preferred_element_type=jnp.float32).reshape(
        seqs, group, width
    )
    grad_shift_two, grad_scale_two, grad_gain_two, grad_normed_two = mod_back(
        grad_hidden_two, ln_two, normed_two, scale_two, vectors[1]
    )
    grad_mid = grad_y + norm_back(normed_two, inv_two, grad_normed_two)
    grad_gate_one = jnp.sum(grad_mid * branch_one, axis=1)
    grad_branch_one = (grad_mid * gate_one).astype(jnp.bfloat16).reshape(flat_rows, width)
    grad_w_attn = jnp.dot(attn_bf.T, grad_branch_one, preferred_element_type=jnp.float32)
    grad_attn_bf = (
        jnp.dot(grad_branch_one, full_attn.T, preferred_element_type=jnp.float32)
        .astype(jnp.bfloat16)
        .reshape(seqs, group, heads, HD)
    )
    delta = jnp.einsum("sqhd,shqd->shq", grad_attn_bf.astype(jnp.float32), attn_heads)
    kv_all = lax.all_gather(kv_local, "seq", axis=1, tiled=True)
    grad_queries = query_grads(kv_all, queries, grad_attn_bf, logsum, delta, width, factor)
    grad_kv = jnp.transpose(
        lax.psum_scatter(
            key_grads(
                kv_all,
                queries,
                grad_attn_bf,
                logsum,
                delta,
                width,
                factor,
                group * lax.axis_size("seq"),
            ).astype(jnp.bfloat16),
            "seq",
            scatter_dimension=0,
            tiled=True,
        ).astype(jnp.float32),
        (1, 0, 2),
    )
    grad_keys = grad_kv[..., :width].reshape(seqs, group, heads, HD)
    grad_qkv = jnp.concatenate(
        [
            rotate_back(grad_queries, cosines, sines).reshape(seqs, group, width),
            rotate_back(grad_keys, cosines, sines).reshape(seqs, group, width),
            grad_kv[..., width:],
        ],
        axis=-1,
    )
    grad_qkv = grad_qkv.astype(jnp.bfloat16).reshape(flat_rows, 3 * width)
    grad_w_qkv = jnp.dot(hidden_one.T, grad_qkv, preferred_element_type=jnp.float32)
    grad_hidden_one = jnp.dot(grad_qkv, full_qkv.T, preferred_element_type=jnp.float32).reshape(
        seqs, group, width
    )
    grad_shift_one, grad_scale_one, grad_gain_one, grad_normed_one = mod_back(
        grad_hidden_one, ln_one, normed_one, scale_one, vectors[0]
    )
    grad_start = grad_mid + norm_back(normed_one, inv_one, grad_normed_one)
    grad_mask_row = jnp.sum(jnp.where(masked[..., None], grad_start, 0.0), axis=(0, 1))
    grad_input = jnp.where(masked[..., None], 0.0, grad_start)
    grad_mod = jnp.concatenate(
        [
            grad_shift_one,
            grad_scale_one,
            grad_gate_one,
            grad_shift_two,
            grad_scale_two,
            grad_gate_two,
        ],
        axis=1,
    )
    grad_w_ada = jnp.dot(cond_bf.astype(jnp.float32).T, grad_mod, precision=lax.Precision.HIGHEST)
    grad_vectors = jnp.concatenate(
        [
            grad_gain_one[None, :],
            grad_gain_two[None, :],
            jnp.sum(grad_mod, axis=0).reshape(6, width),
            grad_mask_row[None, :],
        ],
        axis=0,
    )
    red_ada, red_qkv, red_attn, red_in, red_out, red_vec = (
        lax.psum_scatter(grad_w_ada, ("dp", "seq"), scatter_dimension=1, tiled=True),
        lax.psum_scatter(grad_w_qkv, ("dp", "seq"), scatter_dimension=0, tiled=True),
        lax.psum_scatter(grad_w_attn, ("dp", "seq"), scatter_dimension=0, tiled=True),
        lax.psum_scatter(grad_w_in, ("dp", "seq"), scatter_dimension=0, tiled=True),
        lax.psum_scatter(grad_w_out, ("dp", "seq"), scatter_dimension=0, tiled=True),
        lax.psum_scatter(grad_vectors, ("dp", "seq"), scatter_dimension=1, tiled=True),
    )
    local_squares = jnp.float32(0.0)
    for reduced in (red_vec, red_ada, red_qkv, red_attn, red_in, red_out):
        local_squares = local_squares + jnp.sum(reduced * reduced)
    grad_norm = jnp.sqrt(lax.psum(local_squares, ("dp", "seq")))
    clip_factor = jnp.minimum(1.0, CLIP / (grad_norm + 1e-06))
    columns = red_vec.shape[1]
    own_vectors = lax.dynamic_slice_in_dim(
        vectors, lax.axis_index(("dp", "seq")) * columns, columns, 1
    )
    vec_out = adam_step(own_vectors, red_vec * clip_factor, m_vec, v_vec, RATE_VECTORS, 0.0)
    ada_out = adam_step(w_ada, red_ada * clip_factor, m_ada, v_ada, RATE, DECAY)
    qkv_out = adam_step(w_qkv, red_qkv * clip_factor, m_qkv, v_qkv, RATE, DECAY)
    attn_out = adam_step(w_attn, red_attn * clip_factor, m_attn, v_attn, RATE, DECAY)
    in_out = adam_step(w_in, red_in * clip_factor, m_in, v_in, RATE, DECAY)
    out_out = adam_step(w_out, red_out * clip_factor, m_out, v_out, RATE, DECAY)
    return (
        block_out,
        grad_input,
        grad_norm,
        vec_out[0],
        vec_out[1],
        vec_out[2],
        ada_out[0],
        ada_out[1],
        ada_out[2],
        qkv_out[0],
        qkv_out[1],
        qkv_out[2],
        attn_out[0],
        attn_out[1],
        attn_out[2],
        in_out[0],
        in_out[1],
        in_out[2],
        out_out[0],
        out_out[1],
        out_out[2],
    )


F32, BF = jnp.float32, jnp.bfloat16
MESH = pl.DeviceIdType.MESH
DP, LINE, SEQ, CHIPS, ALL = 4, 4, 8, 16, 32
ROWS, WIDTH, PACK = 128, 768, 640
HALF = WIDTH // 2
HALVES = ((0, 0), (0, 1), (0, 2), (2, 2), (1, 0), (1, 1), (1, 2), None, (2, 0), (2, 1))

def numbered(**counts):
    at = {}
    for name, count in counts.items():
        at[name] = sum(counts[other] for other in at)
    return SimpleNamespace(**at), sum(counts.values())


S, SEM_COUNT = numbered(
    load=11,
    cond=1,
    mix_qkv=1,
    mix_in=1,
    mix_attn=1,
    mod=1,
    w_qkv=1,
    w_attn=4,
    plane_in=1,
    w_in=4,
    w_out=4,
    group_qkv=4,
    group_attn=4,
    fw_qkv=1,
    fw_attn=1,
    fw_in=1,
    fw_out=1,
    tok=4,
    h2=4,
    dm=4,
    xf=4,
    o=1,
    mm=1,
    dh2=1,
    do=1,
    gp=1,
    dh1=5,
    pair_out=1,
    pair_in=1,
    pair_attn=1,
    pair_qkv=1,
    plane_attn=1,
    plane_qkv=1,
    line_out=5,
    line_in=5,
    slice_in=1,
    line_attn=1,
    line_qkv=1,
    last_in=1,
    last_attn=1,
    last_qkv=1,
    early=7,
    late=7,
    sq=1,
)

SCRATCH = dict(
    i_tok=((1, 128, 768), BF),
    i_cot=((1, 128, 768), BF),
    i_vec=((9, 768), F32),
    i_wada=((144, 128), F32),
    i_wqkv=((24, 2304), F32),
    i_wattn=((24, 768), F32),
    i_win=((24, 3072), F32),
    i_wout=((96, 768), F32),
    wide_qkv=((48, 3072), F32),
    wide_in=((48, 3072), F32),
    wide_attn=((48, 768), F32),
    s_qkv=((48, 3072), BF),
    s_in=((48, 3072), BF),
    s_attn=((48, 768), BF),
    w_qkv=((768, 768), BF),
    w_in=((4, 4, 48, 768), BF),
    w_attn=((768, 768), BF),
    w_out=((4, 2, 96, 768), BF),
    t_w_qkv=((640, 768), BF),
    t_w_attn=((768, 1024), BF),
    t_w_in=((768, 768), BF),
    t_w_out=((768, 768), BF),
    t_h1=((768, 512), BF),
    conds_all=((4, 8, 128), F32),
    mod_send=((4, 4, 128), F32),
    mod_got=((32, 4, 128), F32),
    mod_flat=((40, 128), F32),
    mod_pad=((8, 384), F32),
    turn=((2, 4, 128, 128), F32),
    dmod_flat=((4, 40, 128), F32),
    mod=((8, 768), F32),
    x0=((128, 768), F32),
    n1=((4, 128, 768), F32),
    inv1=((4, 128, 128), F32),
    x1=((128, 768), F32),
    n2=((128, 768), F32),
    inv2=((128, 128), F32),
    a=((128, 768), F32),
    dx1=((128, 768), F32),
    toks=((4, 128, 768), BF),
    h1=((4, 128, 768), BF),
    h2=((4, 128, 768), BF),
    dm=((4, 128, 768), BF),
    gb=((4, 128, 768), BF),
    du=((4, 128, 768), BF),
    xb=((2, 4, 128, 640), BF),
    pt=((3, 1024, 512), BF),
    vt=((2, 128, 1024), BF),
    kt=((2, 128, 1024), BF),
    back=((4, 128, 768), F32),
    ot=((2, 128, 512), F32),
    os=((4, 192, 128), BF),
    ob=((4, 192, 128), BF),
    o2=((4, 128, 128), BF),
    mms=((4, 128, 768), BF),
    mmr=((4, 128, 768), BF),
    dhs=((4, 128, 768), BF),
    dhr=((4, 128, 768), BF),
    das=((128, 768), BF),
    dos=((4, 192, 128), BF),
    dob=((4, 192, 128), BF),
    dst=((3, 1024, 512), BF),
    ga=((512, 640), F32),
    gps=((512, 512), BF),
    gpr=((512, 512), BF),
    dqkv=((4, 128, 768), BF),
    d1s=((4, 128, 768), BF),
    d1r=((4, 128, 768), BF),
    g_out=((4, 2, 96, 768), BF),
    g_in=((2, 4, 4, 48, 384), BF),
    g_attn=((2, 768, 384), BF),
    g_qkv=((2, 768, 384), BF),
    p_out=((4, 96, 768), BF),
    p_in=((4, 4, 48, 384), BF),
    p_attn=((768, 384), BF),
    p_qkv=((768, 384), BF),
    q_attn=((4, 192, 384), BF),
    q_qkv=((4, 192, 384), BF),
    m_attn=((192, 384), BF),
    m_qkv=((192, 384), BF),
    r_out=((4, 96, 768), BF),
    r_in=((4, 4, 48, 384), BF),
    via_in=((4, 48, 384), BF),
    via_out=((96, 768), BF),
    via_dh1=((128, 768), BF),
    m_in=((4, 48, 384), BF),
    u_in=((4, 48, 384), BF),
    r_attn=((4, 48, 384), BF),
    r_qkv=((4, 48, 384), BF),
    t_in=((4, 48, 384), F32),
    t_attn=((1, 48, 384), F32),
    t_qkv=((4, 48, 384), F32),
    f_in=((4, 2, 24, 384), F32),
    f_attn=((1, 2, 24, 384), F32),
    f_qkv=((4, 2, 24, 384), F32),
    early=((8, 768), F32),
    early_pair=((8, 768), F32),
    early_line=((4, 8, 384), F32),
    early_plane=((4, 8, 384), F32),
    early_all=((2, 4, 8, 384), F32),
    late=((4, 768), F32),
    late_pair=((4, 768), F32),
    late_line=((4, 4, 384), F32),
    late_plane=((4, 4, 384), F32),
    late_all=((2, 4, 4, 384), F32),
    sq=((32, 1, 128), F32),
)


def dot(left, right):
    return jnp.dot(left, right, preferred_element_type=F32)


def dot_nt(left, right):
    return lax.dot_general(left, right, (((1,), (1,)), ((), ())), preferred_element_type=F32)


def dot_tn(left, right):
    return lax.dot_general(left, right, (((0,), (0,)), ((), ())), preferred_element_type=F32)


def loop(count, body, start=0):
    def step(index, carry):
        body(index)
        return carry

    lax.fori_loop(start, count, step, 0)


def layer_kernel(
    i_time,
    i_start,
    i_len,
    h_tok,
    h_cot,
    h_vec,
    h_wada,
    h_wqkv,
    h_wattn,
    h_win,
    h_wout,
    o_y,
    o_dx,
    o_norm,
    o_gqkv,
    o_gattn,
    o_gin,
    o_gout,
    o_dmod,
    o_gvec,
    o_vec,
    o_conds,
    *scratch,
):
    r = SimpleNamespace(**dict(zip(SCRATCH, scratch)), when=scratch[-3])
    send_sems, recv_sems = scratch[-2:]
    i_tok, i_cot, i_vec, i_wada = r.i_tok, r.i_cot, r.i_vec, r.i_wada
    i_wqkv, i_wattn, i_win, i_wout = r.i_wqkv, r.i_wattn, r.i_win, r.i_wout
    b, s = lax.axis_index("dp"), lax.axis_index("seq")
    z, c = lax.div(s, 2), lax.rem(s, 2)
    mate = s + 1 - 2 * c
    chip = b * LINE + z
    me = b * SEQ + s
    drains = []

    def push(src, dst, at, to_b, to_s, out=None):
        pltpu.make_async_remote_copy(
            src_ref=src,
            dst_ref=dst,
            send_sem=send_sems.at[at if out is None else out],
            recv_sem=recv_sems.at[at],
            device_id=(to_b, to_s),
            device_id_type=MESH,
        ).start()

    def keep(src, dst, at):
        pltpu.make_async_copy(src, dst, recv_sems.at[at]).start()

    def got(at, like):
        pltpu.make_async_copy(like, like, recv_sems.at[at]).wait()

    def left(at, like):
        pltpu.make_async_copy(like, like, send_sems.at[at]).wait()

    def sent(at, like):
        drains.append((at, like))

    near = (b, b + 1 - 2 * lax.rem(b, 2), b + 2 - 4 * lax.div(b, 2), 3 - b)

    def toward(k):
        if k == 3:
            return 3, near[3]
        slot = 1 + c if k == 1 else 2 - c
        return slot, (1 - c) * near[k] + c * near[3 - k]

    def peers(body):
        for k in (1, 2, 3):
            body(*toward(k))

    def stack(body):
        for k in (1, 2, 3):
            body(lax.rem(z + k + 2 * c * (2 - k), LINE))

    def line_gather(block, at, near=True, rest=True):
        inner = 1 + lax.rem(z, 2)
        if near:
            push(block(z), block(z), at + z, b, 2 * inner + c, at)

        def one(to):
            relayed = ((z == 1) & (to == 3)) | ((z == 2) & (to == 0))

            @pl.when(jnp.logical_not(relayed | (to == inner)))
            def _():
                push(block(z), block(z), at + z, b, 2 * to + c, at)

        if rest:
            stack(one)

    def line_relay(block, at):
        for middle, source, to in ((2, 1, 3), (1, 2, 0)):

            @pl.when(z == middle)
            def _():
                got(at + source, block(source))
                push(block(source), block(source), at + source, b, 2 * to + c, at)

    def line_got(block, at, k):
        here = (k == z) | ((z == 2) & (k == 1)) | ((z == 1) & (k == 2))

        @pl.when(jnp.logical_not(here))
        def _():
            got(at + k, block(0))

    far = lax.div(z, 2)

    def line_order(j):
        return lax.rem(z + (2, 3 - 2 * far, 1 + 2 * far, 0)[j], LINE)

    def line_add(j, rows, dst, via, at):
        to = line_order(j)
        outer_chip = (z == 0) | (z == 3)

        def direct():
            push(rows(to), dst.at[z], at + z, b, 2 * to + c, at)

        if j == 0:

            @pl.when(outer_chip)
            def _():
                push(rows(to), via, at + 4, b, 2 * (1 + far) + c, at)

            @pl.when(jnp.logical_not(outer_chip))
            def _():
                direct()

        elif j < 3:
            direct()
        else:
            keep(rows(z), dst.at[z], at + z)

    def line_via(via, at, add):
        @pl.when((z == 1) | (z == 2))
        def _():
            got(at + 4, via)
            add()

    def line_done(dst, at):
        for k in range(4):
            missing = ((z == 1) & (k == 3)) | ((z == 2) & (k == 0))

            @pl.when(jnp.logical_not(missing))
            def _():
                got(at + k, dst.at[k])

    def line_clear(dst):
        for middle, k in ((1, 3), (2, 0)):

            @pl.when(z == middle)
            def _():
                dst[k] = jnp.zeros(dst.shape[1:], BF)

    lane = lax.broadcasted_iota(jnp.int32, (1, 128), 1)
    low = lane < 64
    own24 = pl.ds(pl.multiple_of(24 * c, 8), 24)
    mate24 = pl.ds(pl.multiple_of(24 * (1 - c), 8), 24)
    part = pl.ds(pl.multiple_of(HALF * c, 128), HALF)
    chip_rows = pl.ds(pl.multiple_of(48 * chip, 16), 48)
    group_rows = pl.ds(pl.multiple_of(192 * b, 16), 192)

    barrier = pltpu.get_barrier_semaphore()

    def greet(k):
        other = lax.rem(me + k, ALL)
        pl.semaphore_signal(
            barrier, inc=1, device_id=(lax.div(other, SEQ), lax.rem(other, SEQ)), device_id_type=MESH
        )

    loads = (
        (i_time, r.when.at[0]),
        (i_start, r.when.at[1]),
        (i_len, r.when.at[2]),
        (h_wqkv, i_wqkv),
        (h_win, i_win),
        (h_wattn, i_wattn),
        (h_wout, i_wout),
        (h_tok, i_tok),
        (h_vec, i_vec),
        (h_wada, i_wada),
        (h_cot, i_cot),
    )
    for k, (src, dst) in enumerate(loads):
        pltpu.make_async_copy(src, dst, recv_sems.at[S.load + k]).start()
    loop(ALL, greet, 1)
    for k, (src, dst) in enumerate(loads):
        pltpu.make_async_copy(src, dst, recv_sems.at[S.load + k]).wait()

    def natural(kind, p, head):
        return kind * WIDTH + 192 * p + 64 * head

    def half_at(ref, column, high):
        tile = ref[:, column // 128 * 128 : column // 128 * 128 + 128]
        return tile if (column % 128 == 64) == high else pltpu.roll(tile, 64, 1)

    for p in range(4):
        for tile in range(5):
            pair = []
            for high in (0, 1):
                which = HALVES[2 * tile + high]
                pair.append(
                    jnp.zeros((24, 128), F32)
                    if which is None
                    else half_at(i_wqkv, natural(which[0], p, which[1]), bool(high))
                )
            r.wide_qkv[own24, 768 * p + 128 * tile : 768 * p + 128 * tile + 128] = jnp.where(
                low, pair[0], pair[1]
            )
        r.wide_qkv[own24, 768 * p + 640 : 768 * p + 768] = jnp.zeros((24, 128), F32)
    r.wide_in[own24, :] = i_win[...]
    r.wide_attn[own24, :] = i_wattn[...]
    r.w_out[z, c] = i_wout[...].astype(BF)
    r.toks[z] = i_tok[0]
    line_clear(r.r_out)
    line_clear(r.r_in)
    line_clear(r.d1r)
    lanes8 = lax.broadcasted_iota(jnp.int32, (8, 128), 1)
    half_cond = COND // 2
    speed = jnp.exp((lanes8 % half_cond).astype(F32) * (-math.log(10000.0) / half_cond))
    angle = r.when[0, 0].astype(F32) * speed
    wave = jnp.where(lanes8 < half_cond, jnp.cos(angle), jnp.sin(angle))
    r.conds_all[b] = wave * (1.0 / (1.0 + jnp.exp(-wave)))
    pl.semaphore_wait(barrier, ALL - 1)

    def token_block(k):
        return r.toks.at[k]

    def attn_block(k):
        return r.w_attn.at[pl.ds(pl.multiple_of(192 * b + 48 * k, 16), 48), part]

    def in_block(k):
        return r.w_in.at[:, k, :, part]

    def out_block(k):
        return r.w_out.at[k, c]

    peers(lambda k, to: push(r.conds_all.at[b], r.conds_all.at[b], S.cond, to, s))
    sent(S.cond, r.conds_all.at[0:3])
    push(r.wide_qkv.at[own24], r.wide_qkv.at[own24], S.mix_qkv, b, mate)
    sent(S.mix_qkv, r.wide_qkv.at[0:24])
    push(r.wide_attn.at[own24], r.wide_attn.at[own24], S.mix_attn, b, mate)
    sent(S.mix_attn, r.wide_attn.at[0:24])
    push(r.wide_in.at[own24], r.wide_in.at[own24], S.mix_in, b, mate)
    sent(S.mix_in, r.wide_in.at[0:24])

    got(S.cond, r.conds_all.at[0:3])
    row8 = lax.broadcasted_iota(jnp.int32, (8, 128), 0)
    cond4 = jnp.zeros((8, 128), F32)
    for k in range(4):
        cond4 = jnp.where(row8 == k, r.conds_all[k], cond4)
    o_conds[...] = cond4
    wide = i_wada.shape[0]
    r.mod_pad[...] = jnp.zeros((8, 384), F32)
    r.mod_pad[:, 0:wide] = dot_nt(cond4.astype(BF), i_wada[...].astype(BF))
    columns = pltpu.roll(r.mod_pad[...], lax.rem(wide * me, 128), 1)
    for k in range(4):
        for t in range(3):
            r.mod_send[k, t : t + 1, :] = columns[k : k + 1, 128 * t : 128 * t + 128]
        r.mod_send[k, 3:4, :] = jnp.zeros((1, 128), F32)

    def send_mod(k):
        other = lax.rem(me + k, ALL)
        ob = lax.div(other, SEQ)
        push(r.mod_send.at[ob], r.mod_got.at[me], S.mod, ob, lax.rem(other, SEQ))

    loop(ALL, send_mod, 1)
    sent(S.mod, r.mod_got.at[0:31])
    keep(r.mod_send.at[b], r.mod_got.at[me], S.mod)

    def block(src, first):
        return src.at[:, pl.ds(pl.multiple_of(first, 128), HALF)]

    def along_line(src, dst, at, step):
        stack(
            lambda to: push(
                block(src, step * to + HALF * c), dst.at[chip_rows, part], at, b, 2 * to + c
            )
        )
        keep(block(src, step * z + HALF * c), dst.at[chip_rows, part], at)
        sent(at, dst.at[0:144, 0:HALF])

    def over_plane(dst, at):
        rows = dst.at[group_rows, part]
        peers(lambda k, to: push(rows, rows, at + k, to, s))
        for k in (1, 2, 3):
            sent(at + k, dst.at[0:192, 0:HALF])

    def share(dst, at, onward):
        for k in range(4):
            rows = dst.at[pl.ds(pl.multiple_of(192 * near[k], 16), 192), part]
            if k:
                got(at + k, rows)
            push(rows, rows, onward, b, mate)
        sent(onward, dst.at[:, 0:HALF])

    def line_share(block, at, onward):
        for k in range(4):
            line_got(block, at, k)
            push(block(k), block(k), onward, b, mate)

    got(S.mix_qkv, r.wide_qkv.at[0:24])
    r.s_qkv[...] = r.wide_qkv[...].astype(BF)
    along_line(r.s_qkv, r.w_qkv, S.w_qkv, WIDTH)
    line_gather(token_block, S.tok, rest=False)
    sent(S.tok, r.toks.at[0:3])
    got(S.mix_attn, r.wide_attn.at[0:24])
    r.s_attn[...] = r.wide_attn[...].astype(BF)
    got(S.w_qkv, r.w_qkv.at[0:192, 0:HALF])
    over_plane(r.w_qkv, S.group_qkv)
    line_gather(token_block, S.tok, near=False)
    for h in range(2):

        @pl.when(c == h)
        def _():
            r.w_attn[chip_rows, 384 * h : 384 * h + 384] = r.s_attn[:, 384 * h : 384 * h + 384]

    line_gather(attn_block, S.w_attn)
    sent(S.w_attn, r.w_attn.at[0:144, 0:HALF])
    line_gather(out_block, S.w_out)
    sent(S.w_out, r.w_out.at[0:3, 0])
    got(S.mix_in, r.wide_in.at[0:24])
    r.s_in[...] = r.wide_in[...].astype(BF)
    peers(
        lambda k, to: push(
            block(r.s_in, WIDTH * to + HALF * c), r.w_in.at[b, z, :, part], S.plane_in, to, s
        )
    )
    keep(block(r.s_in, WIDTH * b + HALF * c), r.w_in.at[b, z, :, part], S.plane_in)
    sent(S.plane_in, r.w_in.at[0:3, 0, :, 0:HALF])

    def hidden_rows(k):
        place = (2 * k + c) * ROWS + lax.broadcasted_iota(jnp.int32, (ROWS, 1), 0)
        return (place >= r.when[1, 0]) & (place < r.when[1, 0] + r.when[2, 0])

    def first_norm(tokens, k):
        x0 = jnp.where(hidden_rows(k), i_vec[8:9, :], tokens.astype(F32))
        normed, inverse = normalize(x0)
        r.n1[k] = normed
        r.inv1[k] = jnp.broadcast_to(inverse, (ROWS, 128))
        return x0

    r.x0[...] = first_norm(i_tok[0], z)

    got(S.mod, r.mod_got)
    r.mod_flat[...] = jnp.zeros((40, 128), F32)
    for k in range(ALL):
        first = 9 * k // 8
        r.mod_flat[first : first + 3, :] += r.mod_got[k, 0:3, :]
    for k in range(6):
        row = jnp.concatenate(
            [r.mod_flat[6 * k + t : 6 * k + t + 1, :] for t in range(6)], axis=1
        )
        r.mod[k : k + 1, :] = row + i_vec[2 + k : 3 + k, :]

    def mod(k):
        return r.mod[k : k + 1, :]

    def vec(k):
        return i_vec[k : k + 1, :]

    r.h1[z] = (r.n1[z] * vec(0) * (1.0 + mod(1)) + mod(0)).astype(BF)
    r.dm[0] = (i_cot[0].astype(F32) * mod(5)).astype(BF)
    peers(lambda k, to: push(r.dm.at[0], r.dm.at[k], S.dm + k, to, s))
    for k in (1, 2, 3):
        sent(S.dm + k, r.dm.at[0])

    lanes = lax.broadcasted_iota(jnp.int32, (ROWS, 128), 1)
    first_half = lanes % HD < HD // 2
    speed = jnp.exp((lanes % (HD // 2)).astype(F32) * (-math.log(10000.0) / (HD // 2)))
    row = lax.broadcasted_iota(jnp.int32, (ROWS, 128), 0)

    def table(k):
        angle = ((2 * k + c) * ROWS + row).astype(F32) * speed
        r.turn[0, k] = jnp.cos(angle)
        sine = jnp.sin(angle)
        r.turn[1, k] = jnp.where(first_half, -sine, sine)

    loop(LINE, table)

    line_relay(token_block, S.tok)

    share(r.w_qkv, S.group_qkv, S.fw_qkv)
    got(S.fw_qkv, r.w_qkv.at[:, 0:HALF])
    for k in range(5):
        columns = slice(128 * k, 128 * k + 128)
        r.t_w_qkv[columns, :] = r.w_qkv[:, columns].T

    def turned(tile, sign, k):
        other = jnp.where(first_half, pltpu.roll(tile, 96, 1), pltpu.roll(tile, 32, 1))
        return tile * r.turn[0, k] + sign * (other * r.turn[1, k])

    def project(j):
        k = lax.rem(z + j, LINE)

        @pl.when(j > 0)
        def _():
            line_got(token_block, S.tok, k)
            first_norm(r.toks[k], k)
            r.h1[k] = (r.n1[k] * vec(0) * (1.0 + mod(1)) + mod(0)).astype(BF)

        x = dot(r.h1[k], r.w_qkv[:, 0:PACK])
        tiles = [x[:, 128 * t : 128 * t + 128] for t in range(5)]
        tiles[0] = turned(tiles[0], 1.0, k) * 0.125
        tiles[1] = jnp.where(low, turned(tiles[1], 1.0, k) * 0.125, tiles[1])
        tiles[2] = turned(tiles[2], 1.0, k)
        tiles[3] = turned(tiles[3], 1.0, k)
        for t in range(5):
            r.xb[0, k, :, 128 * t : 128 * t + 128] = tiles[t].astype(BF)
        push(r.xb.at[0, k], r.xb.at[1, k], S.xf + k, b, mate)

    loop(4, project)
    line_relay(attn_block, S.w_attn)
    for k in range(4):
        line_got(attn_block, S.w_attn, k)
    over_plane(r.w_attn, S.group_attn)
    for k in range(4):
        sent(S.xf + k, r.xb.at[0, 0])

    for k in range(6):
        columns = slice(128 * k, 128 * k + 128)
        r.t_h1[columns, :] = r.h1[:, :, columns].reshape(512, 128).T
    for k in range(4):
        got(S.xf + k, r.xb.at[0, 0])

    def tile_of(t):
        return r.xb[:, :, :, 128 * t : 128 * t + 128].reshape(1024, 128)

    heads = ((0, 2, 4, True, True), (0, 2, 4, False, False), (1, 3, 1, True, False))

    def queries(head, first, size):
        q_tile, _, _, q_low, _ = heads[head]
        q = r.xb[0, first : first + size, :, 128 * q_tile : 128 * q_tile + 128]
        return jnp.where(low if q_low else ~low, q.reshape(size * 128, 128), jnp.zeros((), BF))

    r.vt[0] = tile_of(4).T
    r.vt[1] = tile_of(1).T
    for half in range(2):
        at = slice(256 * half, 256 * half + 256)
        for head in range(3):
            scores = dot_nt(tile_of(heads[head][1]), queries(head, 2 * half, 2))
            weights = jnp.exp(scores - jnp.max(scores, axis=0, keepdims=True))
            weights = weights * (1.0 / jnp.sum(weights, axis=0, keepdims=True))
            weights = weights.astype(BF)
            r.pt[head, :, at] = weights
            out = dot(r.vt[head // 2], weights)
            if head == 0:
                r.ot[0, 0:64, at] = out[0:64]
            elif head == 1:
                r.ot[0, 64:128, at] = out[64:128]
            else:
                r.ot[1, 0:64, at] = out[64:128]
                r.ot[1, 64:128, at] = jnp.zeros((64, 256), F32)
        for k in (2 * half, 2 * half + 1):
            across = slice(128 * k, 128 * k + 128)
            r.os[k, 0:128, :] = r.ot[0, :, across].T.astype(BF)
            third = r.ot[1, 0:64, across]
            third = jnp.concatenate([third, pltpu.roll(third, 64, 1)], axis=0)
            r.os[k, 128:192, :] = third.T[0:64].astype(BF)
        for to in (2 * half, 2 * half + 1):

            @pl.when(z == to)
            def _():
                keep(r.os.at[to], r.ob.at[z], S.o)

            @pl.when(z != to)
            def _():
                push(r.os.at[to], r.ob.at[z], S.o, b, 2 * to + c)

        if half == 0:
            line_relay(out_block, S.w_out)

    sent(S.o, r.os.at[0:3])
    got(S.plane_in, r.w_in.at[:, 0, :, 0:HALF])
    line_gather(in_block, S.w_in)
    sent(S.w_in, r.w_in.at[0:3, :, :, 0:HALF])
    for k in range(2):
        r.kt[k] = tile_of(2 + k).T
    share(r.w_attn, S.group_attn, S.fw_attn)
    got(S.fw_attn, r.w_attn.at[:, 0:HALF])
    for p in range(4):
        first = 192 * p
        r.t_w_attn[:, 256 * p : 256 * p + 128] = r.w_attn[first : first + 128, :].T
        third = r.w_attn[first + 128 : first + 192, :]
        r.t_w_attn[:, 256 * p + 128 : 256 * p + 256] = jnp.concatenate(
            [third, jnp.zeros_like(third)], axis=0
        ).T
    got(S.o, r.ob)
    a = jnp.zeros((ROWS, WIDTH), F32)
    for p in range(4):
        third = r.ob[p, 128:192, :].astype(F32)
        third = jnp.concatenate([third, pltpu.roll(third, 64, 1)], axis=0)
        r.o2[p] = jnp.where(low, third, 0.0).astype(BF)
        a += dot(r.ob[p, 0:128, :], r.w_attn[192 * p : 192 * p + 128, :])
        a += dot(r.o2[p, :, 0:64], r.w_attn[192 * p + 128 : 192 * p + 192, :])
    r.a[...] = a
    x1 = r.x0[...] + mod(2) * a
    r.x1[...] = x1
    n2, inv2 = normalize(x1)
    r.n2[...] = n2
    r.inv2[...] = jnp.broadcast_to(inv2, (ROWS, 128))
    r.h2[0] = (n2 * vec(1) * (1.0 + mod(4)) + mod(3)).astype(BF)
    peers(lambda k, to: push(r.h2.at[0], r.h2.at[k], S.h2 + k, to, s))
    for k in (1, 2, 3):
        sent(S.h2 + k, r.h2.at[0])
    line_relay(in_block, S.w_in)
    line_share(out_block, S.w_out, S.fw_out)
    sent(S.fw_out, r.w_out.at[:, 0])
    got(S.fw_out, r.w_out.at[:, 0])

    for k in range(6):
        columns = slice(128 * k, 128 * k + 128)
        r.t_w_out[columns, :] = r.w_out[:, :, :, columns].reshape(WIDTH, 128).T

    def feed_back(k):
        @pl.when(k > 0)
        def _():
            got(S.dm + k, r.dm.at[0])

        r.back[k] = dot(r.dm[k], r.t_w_out[...])

    loop(4, feed_back)
    line_share(in_block, S.w_in, S.fw_in)
    sent(S.fw_in, r.w_in.at[:, :, :, 0:HALF])
    got(S.fw_in, r.w_in.at[:, :, :, 0:HALF])
    for k in range(6):
        columns = slice(128 * k, 128 * k + 128)
        r.t_w_in[columns, :] = r.w_in[:, :, :, columns].reshape(WIDTH, 128).T

    def feed(first, count):
        at = slice(first, first + count)
        size = count * ROWS
        u = dot(r.h2[at].reshape(size, WIDTH), r.w_in[...].reshape(WIDTH, WIDTH))
        slope = 0.7978845608028654
        cube = 0.044715
        t = jnp.tanh(slope * (u + cube * u * u * u))
        r.gb[at] = (0.5 * u * (1.0 + t)).astype(BF).reshape(count, ROWS, WIDTH)
        bend = 0.5 * (1.0 + t) + 0.5 * u * (1.0 - t * t) * (slope * (1.0 + 3.0 * cube * u * u))
        du = (r.back[at].reshape(size, WIDTH) * bend).astype(BF)
        r.du[at] = du.reshape(count, ROWS, WIDTH)
        r.dhs[at] = dot(du, r.t_w_in[...]).astype(BF).reshape(count, ROWS, WIDTH)

    feed(0, 1)
    for first, count in ((1, 2), (3, 1)):
        for k in range(first, first + count):
            got(S.h2 + k, r.h2.at[0])
        feed(first, count)
        for k in range(first, first + count):
            slot, to = toward(k)
            push(r.dhs.at[slot], r.dhr.at[slot], S.dh2, to, s)
    sent(S.dh2, r.dhs.at[0:3])
    def gather(own, others):
        total = own[0].astype(F32)
        for k in (1, 2, 3):
            total += others[k].astype(F32)
        return total

    for k in range(2):
        rows = slice(384 * k, 384 * k + 384)
        result = dot_tn(r.gb[:, :, rows].reshape(512, 384), r.dm[...].reshape(512, 768))
        r.g_out[2 * k : 2 * k + 2] = result.astype(BF).reshape(2, 2, 96, 768)
    push(r.g_out.at[:, 1 - c], r.p_out, S.pair_out, b, mate)
    sent(S.pair_out, r.p_out)

    def to_mate(grad, dst, at):
        push(grad.at[1 - c], dst, at, b, mate)
        sent(at, dst)

    def pair_sum(grad, pair, at):
        got(at, pair)
        grad[c] = (grad[c].astype(F32) + pair[...].astype(F32)).astype(BF)

    def plane_sum(grad, dst, at):
        def rows(to):
            return grad.at[c, pl.ds(pl.multiple_of(192 * to, 16), 192)]

        peers(lambda k, to: push(rows(to), dst.at[k], at, to, s))
        keep(rows(b), dst.at[0], at)
        sent(at, dst.at[0:3])

    def line_sum(src, total, dst, first, at):
        got(first, src)
        total[...] = (
            (src[0].astype(F32) + src[1].astype(F32)) + (src[2].astype(F32) + src[3].astype(F32))
        ).astype(BF)

        def rows(to):
            return total.at[pl.ds(pl.multiple_of(48 * to, 16), 48)]

        stack(lambda to: push(rows(to), dst.at[z], at, b, 2 * to + c))
        keep(rows(z), dst.at[z], at)
        sent(at, dst.at[0:3])

    def trade(total, final, at):
        push(total.at[:, mate24], final.at[:, c], at, b, mate)
        sent(at, final.at[:, 0])
        final[:, c] = total[:, own24, :]

    def in_product(k):
        rows = slice(384 * k, 384 * k + 384)
        result = dot_tn(r.h2[:, :, rows].reshape(512, 384), r.du[...].reshape(512, 768)).astype(BF)
        for h in range(2):
            r.g_in[h, 2 * k : 2 * k + 2] = result[:, 384 * h : 384 * h + 384].reshape(2, 4, 48, 384)

    in_product(0)

    got(S.pair_out, r.p_out)
    for k in range(4):
        r.g_out[k, c] = (r.g_out[k, c].astype(F32) + r.p_out[k].astype(F32)).astype(BF)

    def out_rows(k):
        return r.g_out.at[k, c]

    for j in (0, 1):
        line_add(j, out_rows, r.r_out, r.via_out, S.line_out)
    in_product(1)
    to_mate(r.g_in, r.p_in, S.pair_in)

    def add_out():
        k = line_order(2)
        r.g_out[k, c] = (r.g_out[k, c].astype(F32) + r.via_out[...].astype(F32)).astype(BF)

    got(S.dh2, r.dhr.at[0:3])
    dh = gather(r.dhs, r.dhr)
    n2 = r.n2[...]
    inv2 = r.inv2[:, 0:1]
    r.early[...] = jnp.zeros((8, 768), F32)
    r.early[2:3, :] = jnp.sum(dh, axis=0, keepdims=True)
    both = jnp.sum(dh * n2, axis=0, keepdims=True)
    r.early[3:4, :] = both * vec(1)
    r.early[0:1, :] = both * (1.0 + mod(4))
    grad = dh * ((1.0 + mod(4)) * vec(1))
    dx1 = i_cot[0].astype(F32) + norm_back(n2, inv2, grad)
    r.dx1[...] = dx1
    r.early[1:2, :] = jnp.sum(dx1 * r.a[...], axis=0, keepdims=True)
    r.das[...] = (dx1 * mod(2)).astype(BF)
    for p in range(4):
        result = dot(r.das[...], r.t_w_attn[:, 256 * p : 256 * p + 256])
        r.dos[p, 0:128, :] = result[:, 0:128].astype(BF)
        third = result[:, 128:256]
        third = jnp.where(low, third[0:64], pltpu.roll(third[64:128], 64, 1))
        r.dos[p, 128:192, :] = third.astype(BF)
    stack(lambda to: push(r.dos.at[to], r.dob.at[z], S.do, b, 2 * to + c))
    keep(r.dos.at[z], r.dob.at[z], S.do)
    sent(S.do, r.dos.at[0:3])
    for t in range(3):
        at = slice(256 * t, 256 * t + 256)
        mm = dot(r.gb[...].reshape(512, WIDTH), r.w_out[:, :, :, at].reshape(WIDTH, 256))
        r.mms[:, :, at] = mm.astype(BF).reshape(4, ROWS, 256)
    peers(lambda k, to: push(r.mms.at[k], r.mmr.at[k], S.mm, to, s))
    sent(S.mm, r.mms.at[0:3])

    for p in range(4):
        for rows, left_side in (
            (slice(192 * p, 192 * p + 128), r.ob[p, 0:128, :]),
            (slice(192 * p + 128, 192 * p + 192), r.o2[p]),
        ):
            result = dot_tn(left_side, r.das[...])[0 : rows.stop - rows.start].astype(BF)
            r.g_attn[0, rows, :] = result[:, 0:HALF]
            r.g_attn[1, rows, :] = result[:, HALF:WIDTH]
    to_mate(r.g_attn, r.p_attn, S.pair_attn)

    def small_sum(src, pair, line, plane, whole, at):
        def first():
            push(src, pair, at, b, mate)
            sent(at, src)

        def second():
            got(at, pair)
            total = src[...] + pair[...]
            line[z] = (1 - c) * total[:, 0:HALF] + c * total[:, HALF:WIDTH]
            stack(lambda to: push(line.at[z], line.at[z], at + 1, b, 2 * to + c))
            sent(at + 1, line.at[0:3])

        def third():
            got(at + 1, line.at[0:3])
            plane[b] = (line[0] + line[1]) + (line[2] + line[3])
            peers(lambda k, to: push(plane.at[b], plane.at[b], at + 2, to, s))
            sent(at + 2, plane.at[0:3])

        def fourth():
            got(at + 2, plane.at[0:3])
            whole[c] = plane[...]
            push(plane, whole.at[c], at + 3, b, mate)
            sent(at + 3, plane)

        def rows(k):
            return jnp.concatenate([whole[0, k], whole[1, k]], axis=1)

        return first, second, third, fourth, rows

    early_steps = small_sum(
        r.early, r.early_pair, r.early_line, r.early_plane, r.early_all, S.early
    )
    late_steps = small_sum(r.late, r.late_pair, r.late_line, r.late_plane, r.late_all, S.late)

    pair_sum(r.g_in, r.p_in, S.pair_in)
    line_via(r.via_out, S.line_out, add_out)
    for j in (2, 3):
        line_add(j, out_rows, r.r_out, r.via_out, S.line_out)
    sent(S.line_out, r.r_out.at[0:3])

    def in_rows(k):
        return r.g_in.at[c, :, k]

    for j in (0, 1):
        line_add(j, in_rows, r.r_in, r.via_in, S.line_in)

    def add_in():
        k = line_order(2)
        r.g_in[c, :, k] = (r.g_in[c, :, k].astype(F32) + r.via_in[...].astype(F32)).astype(BF)

    pair_sum(r.g_attn, r.p_attn, S.pair_attn)
    plane_sum(r.g_attn, r.q_attn, S.plane_attn)

    got(S.do, r.dob)
    dot0 = r.dob[:, 0:128, :].reshape(512, 128)
    third = r.dob[:, 128:192, :].astype(F32).reshape(256, 128)
    other_rows = jnp.where(low, pltpu.roll(third, 64, 1), 0.0).reshape(4, 64, 128)
    third = jnp.where(low, third, 0.0).reshape(4, 64, 128)
    dot1 = jnp.concatenate([third, other_rows], axis=1).reshape(512, 128)
    zero = jnp.zeros((), BF)
    moved = pltpu.roll(dot1, 64, 1).astype(BF)
    grads = (jnp.where(low, dot0, zero), jnp.where(low, zero, dot0), moved)
    product = dot0.astype(F32).T * r.ot[0]
    deltas = (
        jnp.sum(product[0:64], axis=0, keepdims=True),
        jnp.sum(product[64:128], axis=0, keepdims=True),
        jnp.sum(dot1.T * r.ot[1], axis=0, keepdims=True),
    )
    for head in range(3):
        values = tile_of(heads[head][2])
        for half in range(2):
            at = slice(256 * half, 256 * half + 256)
            dp = dot_nt(values, grads[head][at])
            r.dst[head, :, at] = (
                r.pt[head, :, at].astype(F32) * (dp - deltas[head][:, at])
            ).astype(BF)

    def key_grads(rows):
        dk = [dot(r.dst[head, rows, :], queries(head, 0, 4)) for head in range(3)]
        dv = [dot(r.pt[head, rows, :], grads[head]) for head in range(3)]
        return (dv[2], dk[0] + dk[1], dk[2], dv[0] + dv[1])

    line_via(r.via_in, S.line_in, add_in)
    for j in (2, 3):
        line_add(j, in_rows, r.r_in, r.via_in, S.line_in)
    sent(S.line_in, r.r_in.at[0:3])
    for t, tile in enumerate(key_grads(slice(512, 1024))):
        r.gps[:, 128 * t : 128 * t + 128] = tile.astype(BF)
    push(r.gps, r.gpr, S.gp, b, mate)
    sent(S.gp, r.gps)
    for t, tile in enumerate(key_grads(slice(0, 512))):
        r.ga[:, 128 * t + 128 : 128 * t + 256] = tile
    for half in range(2):
        at = slice(256 * half, 256 * half + 256)
        turned_q = [dot(r.kt[head // 2], r.dst[head, :, at]) for head in range(3)]
        top = jnp.concatenate([turned_q[0][0:64], turned_q[1][64:128]], axis=0)
        r.ga[at, 0:128] = top.T * 0.125
        r.ga[at, 128:256] += turned_q[2].T * 0.125
    got(S.mm, r.mmr.at[0:3])
    mm = gather(r.mms, r.mmr)
    o_y[...] = (r.x1[...] + mod(5) * mm).astype(BF)
    r.early[4:5, :] = jnp.sum(i_cot[0].astype(F32) * mm, axis=0, keepdims=True)
    early_steps[0]()
    got(S.gp, r.gpr)

    def dh1_rows(k):
        return r.d1s.at[k]

    def back_turn(k):
        rows = pl.ds(pl.multiple_of(128 * k, 128), 128)
        tiles = [r.ga[rows, 0:128]] + [
            r.ga[rows, 128 * t : 128 * t + 128]
            + r.gpr[rows, 128 * t - 128 : 128 * t].astype(F32)
            for t in range(1, 5)
        ]
        tiles[0] = turned(tiles[0], -1.0, k)
        tiles[1] = jnp.where(low, turned(tiles[1], -1.0, k), tiles[1])
        tiles[2] = turned(tiles[2], -1.0, k)
        tiles[3] = turned(tiles[3], -1.0, k)
        for t in range(5):
            r.dqkv[k, :, 128 * t : 128 * t + 128] = tiles[t].astype(BF)
        r.dqkv[k, :, PACK:WIDTH] = jnp.zeros((128, 128), BF)

    loop(4, back_turn)
    early_steps[1]()

    def unproject(j):
        k = line_order(j)
        partial_sum = dot(r.dqkv[k, :, 0:PACK], r.t_w_qkv[...])
        r.d1s[k] = partial_sum.astype(BF)
        if j == 2:

            def add():
                r.d1s[k] = (partial_sum + r.via_dh1[...].astype(F32)).astype(BF)

            line_via(r.via_dh1, S.dh1, add)
        line_add(j, dh1_rows, r.d1r, r.via_dh1, S.dh1)
        n = r.n1[k]
        e = partial_sum * ((1.0 + mod(1)) * vec(0))
        weight = jnp.where(hidden_rows(k), r.inv1[k][:, 0:1], 0.0)
        centred = (
            e
            - jnp.mean(e, axis=-1, keepdims=True)
            - n * jnp.mean(e * n, axis=-1, keepdims=True)
        )
        r.late[0:1, :] += jnp.sum(partial_sum * n, axis=0, keepdims=True)
        r.late[1:2, :] += jnp.sum(partial_sum, axis=0, keepdims=True)
        r.late[3:4, :] += jnp.sum(weight * centred, axis=0, keepdims=True)

    r.late[...] = jnp.zeros((4, 768), F32)
    r.late[3:4, :] = jnp.sum(
        jnp.where(hidden_rows(z), r.dx1[...], 0.0), axis=0, keepdims=True
    )
    unproject(0)

    def qkv_rows(k):
        rows = pl.ds(pl.multiple_of(128 * k, 128), 128)
        result = dot(r.t_h1[rows, :], r.dqkv[...].reshape(512, WIDTH)).astype(BF)
        r.g_qkv[0, rows, :] = result[:, 0:HALF]
        r.g_qkv[1, rows, :] = result[:, HALF:WIDTH]

    loop(6, qkv_rows)
    to_mate(r.g_qkv, r.p_qkv, S.pair_qkv)
    unproject(1)
    pair_sum(r.g_qkv, r.p_qkv, S.pair_qkv)
    plane_sum(r.g_qkv, r.q_qkv, S.plane_qkv)
    early_steps[2]()
    unproject(2)
    unproject(3)
    sent(S.dh1, r.d1s.at[0:3])
    both = r.late[0:1, :]
    r.late[2:3, :] = both * vec(0)
    r.late[0:1, :] = both * (1.0 + mod(1))
    late_steps[0]()
    early_steps[3]()
    line_sum(r.q_attn, r.m_attn, r.r_attn, S.plane_attn, S.line_attn)
    late_steps[1]()

    line_done(r.r_in, S.line_in)
    r.m_in[...] = (
        (r.r_in[0].astype(F32) + r.r_in[1].astype(F32))
        + (r.r_in[2].astype(F32) + r.r_in[3].astype(F32))
    ).astype(BF)
    peers(lambda k, to: push(r.m_in.at[to], r.u_in.at[b], S.slice_in, to, s))
    keep(r.m_in.at[b], r.u_in.at[b], S.slice_in)
    sent(S.slice_in, r.u_in.at[0:3])
    line_sum(r.q_qkv, r.m_qkv, r.r_qkv, S.plane_qkv, S.line_qkv)
    late_steps[2]()

    line_done(r.d1r, S.dh1)
    dh = (r.d1r[0].astype(F32) + r.d1r[1].astype(F32)) + (
        r.d1r[2].astype(F32) + r.d1r[3].astype(F32)
    )
    n1 = r.n1[z]
    grad = dh * ((1.0 + mod(1)) * vec(0))
    dx0 = r.dx1[...] + norm_back(n1, r.inv1[z][:, 0:1], grad)
    o_dx[...] = jnp.where(hidden_rows(z), 0.0, dx0)
    late_steps[3]()

    line_done(r.r_out, S.line_out)
    total = (r.r_out[0].astype(F32) + r.r_out[1].astype(F32)) + (
        r.r_out[2].astype(F32) + r.r_out[3].astype(F32)
    )
    o_gout[...] = total
    squares = total * total
    squares = jnp.sum(squares[:, 0:128] + squares[:, 128:256] + squares[:, 256:384]
                      + squares[:, 384:512] + squares[:, 512:640] + squares[:, 640:768],
                      axis=0, keepdims=True)

    def fold(value):
        total = value[:, 0:128] * value[:, 0:128]
        for t in range(1, value.shape[1] // 128):
            total += value[:, 128 * t : 128 * t + 128] * value[:, 128 * t : 128 * t + 128]
        return jnp.sum(total, axis=0, keepdims=True)

    got(S.slice_in, r.u_in)
    r.t_in[...] = r.u_in[...].astype(F32)
    for p in range(4):
        squares += fold(r.t_in[p])
    trade(r.t_in, r.f_in, S.last_in)
    got(S.line_attn, r.r_attn)
    r.t_attn[0] = (r.r_attn[0].astype(F32) + r.r_attn[1].astype(F32)) + (
        r.r_attn[2].astype(F32) + r.r_attn[3].astype(F32)
    )
    squares += fold(r.t_attn[0])
    trade(r.t_attn, r.f_attn, S.last_attn)
    got(S.line_qkv, r.r_qkv)
    r.t_qkv[...] = r.r_qkv[...].astype(F32)
    trade(r.t_qkv, r.f_qkv, S.last_qkv)
    for p in range(4):
        squares += fold(r.t_qkv[p])
    r.sq[me] = squares

    def send_sq(k):
        other = lax.rem(me + k, ALL)
        push(r.sq.at[me], r.sq.at[me], S.sq, lax.div(other, SEQ), lax.rem(other, SEQ))

    loop(ALL, send_sq, 1)
    sent(S.sq, r.sq.at[0:31])
    got(S.last_in, r.f_in.at[:, 0])
    got(S.last_attn, r.f_attn.at[:, 0])
    for h in range(2):
        for p in range(4):
            value = r.f_in[p, h]
            o_gin[:, 768 * p + 384 * h : 768 * p + 384 * h + 384] = value
        value = r.f_attn[0, h]
        o_gattn[:, 384 * h : 384 * h + 384] = value
    got(S.last_qkv, r.f_qkv.at[:, 0])
    where = {which: index for index, which in enumerate(HALVES) if which is not None}

    def packed_half(chunk, high):
        kind, rest = chunk // 12, chunk % 12
        index = where[(kind, rest % 3)]
        t = index // 2
        tile = r.f_qkv[rest // 3, t // 3, :, t % 3 * 128 : t % 3 * 128 + 128]
        return tile if index % 2 == high else pltpu.roll(tile, 64, 1)

    for t in range(18):
        o_gqkv[:, 128 * t : 128 * t + 128] = jnp.where(
            low, packed_half(2 * t, 0), packed_half(2 * t + 1, 1)
        )
    got(S.early + 3, r.early_all.at[0])
    got(S.late + 3, r.late_all.at[0])
    early_rows = [early_steps[4](k) for k in range(4)]
    late_rows = [late_steps[4](k) for k in range(4)]
    mods = []
    for k in range(4):
        early, late = early_rows[k], late_rows[k]
        rows = jnp.concatenate([late[1:3], early[1:5], jnp.zeros((2, 768), F32)], axis=0)
        for n in range(6):
            for m in range(6):
                r.dmod_flat[k, 6 * n + m : 6 * n + m + 1, :] = rows[
                    n : n + 1, 128 * m : 128 * m + 128
                ]
        mods.append(rows)
    gain = jnp.concatenate(
        [
            sum(late_rows[k][0:1] for k in range(4)),
            sum(early_rows[k][0:1] for k in range(4)),
            (mods[0] + mods[1] + mods[2] + mods[3])[0:6],
        ],
        axis=0,
    )
    mask_row = sum(late_rows[k][3:4] for k in range(4))
    gains = jnp.concatenate([gain, mask_row, jnp.zeros((7, 768), F32)], axis=0)
    masters = jnp.concatenate([i_vec[...], jnp.zeros((7, 768), F32)], axis=0)
    own = lax.rem(WIDTH - 24 * me, WIDTH)
    o_gvec[...] = pltpu.roll(gains, own, 1)[:, 0:128]
    o_vec[...] = pltpu.roll(masters, own, 1)[:, 0:128]
    r.mod_pad[...] = jnp.zeros((8, 384), F32)
    window = lax.div(wide * me, 128)
    for k in range(4):
        rows = r.dmod_flat[k, pl.ds(window, 3), :]
        for m in range(3):
            r.mod_pad[k : k + 1, 128 * m : 128 * m + 128] = rows[m : m + 1, :]
    o_dmod[...] = pltpu.roll(r.mod_pad[...], lax.rem(384 - lax.rem(wide * me, 128), 384), 1)[:, 0:256]
    small = jnp.sum(gain * gain) + jnp.sum(mask_row * mask_row)
    conds = [r.conds_all[k][0:1].astype(BF).astype(F32) for k in range(4)]
    for k in range(4):
        for m in range(k, 4):
            term = jnp.sum(mods[k] * mods[m]) * jnp.sum(conds[k] * conds[m])
            small += term if m == k else 2.0 * term
    got(S.sq, r.sq.at[0:31])
    total = r.sq[0]
    for k in range(1, ALL):
        total += r.sq[k]
    o_norm[...] = jnp.broadcast_to(jnp.sqrt(jnp.sum(total) + small), (8, 128))

    for at, like in drains:
        left(at, like)


def run_layer(*args):
    shapes = (
        ((ROWS, WIDTH), BF),
        ((ROWS, WIDTH), F32),
        ((8, 128), F32),
        ((24, 3 * WIDTH), F32),
        ((24, WIDTH), F32),
        ((24, 4 * WIDTH), F32),
        ((96, WIDTH), F32),
        ((8, 256), F32),
        ((16, 128), F32),
        ((16, 128), F32),
        ((8, 128), F32),
    )
    whole = pl.BlockSpec(memory_space=pltpu.VMEM)
    return pl.pallas_call(
        layer_kernel,
        out_shape=[jax.ShapeDtypeStruct(shape, kind) for shape, kind in shapes],
        in_specs=[pl.BlockSpec(memory_space=pl.ANY)] * len(args),
        out_specs=[whole] * len(shapes),
        scratch_shapes=[pltpu.VMEM(shape, kind) for shape, kind in SCRATCH.values()]
        + [pltpu.SMEM((3, 1), jnp.int32)]
        + [pltpu.SemaphoreType.DMA((SEM_COUNT,)), pltpu.SemaphoreType.DMA((SEM_COUNT,))],
        compiler_params=pltpu.CompilerParams(
            collective_id=0, has_side_effects=True, vmem_limit_bytes=60 * 1024 * 1024
        ),
    )(*args)


HELD = (2, 8, 9, 7, 10, 3, 4, 5, 6)


def finish_kernel(*refs):
    sources, outs, refs = refs[:28], refs[28:49], refs[49:]
    near, results, load_sems, store_sems = refs[:26], refs[26:44], refs[44], refs[45]
    norm, g_vec, own_vec, dmod, conds = near[:5]
    weights, moments = (own_vec, *near[9:14]), near[14:]

    order = list(range(5)) + [14, 15, 9, 16, 17]
    for k in range(2, 6):
        order += [3 + k, 8 + k, 14 + 2 * k, 15 + 2 * k]
    loads = {}
    for n in order:
        source = sources[HELD[n]] if n < 9 else sources[n + 2]
        loads[n] = pltpu.make_async_copy(source, near[n], load_sems.at[n])
        loads[n].start()
    through = [
        pltpu.make_async_copy(sources[k], outs[k].at[0], store_sems.at[18 + k]) for k in range(2)
    ]
    for copy in through:
        copy.start()
    for n in order[:10]:
        loads[n].wait()
    outs[2][0, 0] = norm[0, 0]
    clip = jnp.minimum(1.0, CLIP / (norm[0:1, 0:1] + 1e-06))
    wide, narrow = near[9].shape[0], moments[0].shape[1]
    rounded = conds[...].astype(BF).astype(F32)
    turned_mod = dmod[...].T
    g_ada = turned_mod[0:wide, 0:1] * rounded[0:1, :]
    for k in range(1, 4):
        g_ada += turned_mod[0:wide, k : k + 1] * rounded[k : k + 1, :]
    stores = []
    for k in range(6):
        if k > 1:
            for n in order[2 + 4 * k : 6 + 4 * k]:
                loads[n].wait()
        grad = g_vec[0:9, 0:narrow] if k == 0 else g_ada if k == 1 else near[3 + k][...]
        updated = adam_step(
            weights[k][...] if k else own_vec[0:9, 0:narrow],
            grad * clip,
            moments[2 * k][...],
            moments[2 * k + 1][...],
            RATE if k else RATE_VECTORS,
            DECAY if k else 0.0,
        )
        for n in range(3):
            at = 3 * k + n
            results[at][...] = updated[n]
            stores.append(pltpu.make_async_copy(results[at], outs[3 + at], store_sems.at[at]))
            stores[-1].start()
    for copy in through + stores:
        copy.wait()


def run_finish(partial_results, weights, moments):
    shapes = [((1, ROWS, WIDTH), BF), ((1, ROWS, WIDTH), F32), ((1, 1), F32)]
    for moment in moments[::2]:
        shapes += [(moment.shape, F32)] * 3
    far = pl.BlockSpec(memory_space=pl.ANY)
    specs = [far] * len(shapes)
    specs[2] = pl.BlockSpec(memory_space=pltpu.SMEM)
    near = [partial_results[k] for k in HELD] + [*weights, *moments]
    args = (*partial_results, *weights, *moments)
    return pl.pallas_call(
        finish_kernel,
        out_shape=[jax.ShapeDtypeStruct(shape, kind) for shape, kind in shapes],
        in_specs=[far] * len(args),
        out_specs=specs,
        scratch_shapes=[pltpu.VMEM(array.shape, array.dtype) for array in near]
        + [pltpu.VMEM(shape, kind) for shape, kind in shapes[3:]]
        + [pltpu.SemaphoreType.DMA((26,)), pltpu.SemaphoreType.DMA((20,))],
        compiler_params=pltpu.CompilerParams(vmem_limit_bytes=60 * 1024 * 1024),
    )(*args)


def slices(
    tokens_in,
    cotangent,
    timesteps,
    span_start,
    span_len,
    vectors,
    w_ada,
    w_qkv,
    w_attn,
    w_in,
    w_out,
    m_vec,
    v_vec,
    m_ada,
    v_ada,
    m_qkv,
    v_qkv,
    m_attn,
    v_attn,
    m_in,
    v_in,
    m_out,
    v_out,
):
    partial_results = run_layer(
        timesteps,
        span_start,
        span_len,
        tokens_in,
        cotangent,
        vectors,
        w_ada.T,
        w_qkv,
        w_attn,
        w_in,
        w_out,
    )
    moments = (
        m_vec,
        v_vec,
        m_ada.T,
        v_ada.T,
        m_qkv,
        v_qkv,
        m_attn,
        v_attn,
        m_in,
        v_in,
        m_out,
        v_out,
    )
    results = run_finish(partial_results, (w_ada.T, w_qkv, w_attn, w_in, w_out), moments)
    ada_results = [result.T for result in results[6:9]]
    return (*results[:2], results[2].reshape(()), *results[3:6], *ada_results, *results[9:])


def solution(mesh):
    in_specs = (
        P("dp", "seq", None),
        P("dp", "seq", None),
        P("dp"),
        P("dp"),
        P("dp"),
        P(),
        P(None, ("dp", "seq")),
        P(("dp", "seq"), None),
        P(("dp", "seq"), None),
        P(("dp", "seq"), None),
        P(("dp", "seq"), None),
        P(None, ("dp", "seq")),
        P(None, ("dp", "seq")),
        P(None, ("dp", "seq")),
        P(None, ("dp", "seq")),
        P(("dp", "seq"), None),
        P(("dp", "seq"), None),
        P(("dp", "seq"), None),
        P(("dp", "seq"), None),
        P(("dp", "seq"), None),
        P(("dp", "seq"), None),
        P(("dp", "seq"), None),
        P(("dp", "seq"), None),
    )
    out_specs = (
        P("dp", "seq", None),
        P("dp", "seq", None),
        P(),
        P(None, ("dp", "seq")),
        P(None, ("dp", "seq")),
        P(None, ("dp", "seq")),
        P(None, ("dp", "seq")),
        P(None, ("dp", "seq")),
        P(None, ("dp", "seq")),
        P(("dp", "seq"), None),
        P(("dp", "seq"), None),
        P(("dp", "seq"), None),
        P(("dp", "seq"), None),
        P(("dp", "seq"), None),
        P(("dp", "seq"), None),
        P(("dp", "seq"), None),
        P(("dp", "seq"), None),
        P(("dp", "seq"), None),
        P(("dp", "seq"), None),
        P(("dp", "seq"), None),
        P(("dp", "seq"), None),
    )
    sizes = dict(mesh.shape)
    local = slices if (sizes["dp"], sizes["seq"]) == (4, 8) else plain
    return jax.shard_map(local, mesh=mesh, in_specs=in_specs, out_specs=out_specs, check_vma=False)
```

```python
from functools import partial
import math
from types import SimpleNamespace

import jax
import jax.numpy as jnp
from jax import lax
from jax.experimental import pallas as pl
from jax.experimental.pallas import tpu as pltpu
from jax.sharding import PartitionSpec as P

HD = 64
COND = 128
STEP = 10


BETA_ONE = 0.9
BETA_TWO = 0.999
ADAM_EPS = 1e-08
RATE = 0.1
RATE_VECTORS = 0.3
DECAY = 0.01
CLIP = 1.0
NORM_EPS = 1e-05


def cond_input(timesteps):
    half_cond = COND // 2
    freqs = jnp.exp(jnp.arange(half_cond, dtype=jnp.float32) * (-math.log(10000.0) / half_cond))
    angles = timesteps.astype(jnp.float32)[:, None] * freqs[None, :]
    return jax.nn.silu(jnp.concatenate([jnp.cos(angles), jnp.sin(angles)], axis=1))


def rotary_tables(positions):
    half_head = HD // 2
    inverse = jnp.exp(jnp.arange(half_head, dtype=jnp.float32) * (-math.log(10000.0) / half_head))
    angles = positions.astype(jnp.float32)[:, None] * inverse[None, :]
    return (jnp.cos(angles), jnp.sin(angles))


def rotate(values, cosines, sines):
    half_head = values.shape[-1] // 2
    first = values[..., :half_head]
    second = values[..., half_head:]
    cos_b = cosines[:, None, :]
    sin_b = sines[:, None, :]
    return jnp.concatenate(
        [first * cos_b - second * sin_b, second * cos_b + first * sin_b], axis=-1
    )


def rotate_back(grads, cosines, sines):
    half_head = grads.shape[-1] // 2
    first = grads[..., :half_head]
    second = grads[..., half_head:]
    cos_b = cosines[:, None, :]
    sin_b = sines[:, None, :]
    return jnp.concatenate(
        [first * cos_b + second * sin_b, second * cos_b - first * sin_b], axis=-1
    )


def normalize(values):
    centre = jnp.mean(values, axis=-1, keepdims=True)
    centred = values - centre
    inverse = lax.rsqrt(jnp.mean(centred * centred, axis=-1, keepdims=True) + NORM_EPS)
    return (centred * inverse, inverse)


def norm_back(normed, inverse, grad):
    return inverse * (
        grad
        - jnp.mean(grad, axis=-1, keepdims=True)
        - normed * jnp.mean(grad * normed, axis=-1, keepdims=True)
    )


def split_kv(block, width):
    seqs, block_rows = (block.shape[0], block.shape[1])
    keys = block[..., :width].reshape(seqs, block_rows, width // HD, HD)
    values = block[..., width:].reshape(seqs, block_rows, width // HD, HD)
    return (keys, values)


def attend_piece(carry, piece, queries, width, factor):
    piece_rows = piece.shape[1]
    size = math.gcd(piece_rows, 512)

    def attend_one_block(index, state):
        running, denom, accum = state
        block = lax.dynamic_slice_in_dim(piece, index * size, size, 1)
        keys, values = split_kv(block, width)
        scores = (
            jnp.einsum("sqhd,skhd->shqk", queries, keys, preferred_element_type=jnp.float32)
            * factor
        )
        highest = jnp.maximum(running, jnp.max(scores, axis=-1))
        shrink = jnp.exp(running - highest)
        weights = jnp.exp(scores - highest[..., None])
        denom = denom * shrink + jnp.sum(weights, axis=-1)
        accum = accum * shrink[..., None] + jnp.einsum(
            "shqk,skhd->shqd",
            weights.astype(jnp.bfloat16),
            values,
            preferred_element_type=jnp.float32,
        )
        return (highest, denom, accum)

    return lax.fori_loop(0, piece_rows // size, attend_one_block, carry)


def block_grads(block, queries, grad_out, logsum, delta, width, factor):
    keys, values = split_kv(block, width)
    scores = (
        jnp.einsum("sqhd,skhd->shqk", queries, keys, preferred_element_type=jnp.float32) * factor
    )
    probs = jnp.exp(scores - logsum[..., None])
    dprobs = jnp.einsum("sqhd,skhd->shqk", grad_out, values, preferred_element_type=jnp.float32)
    dscores = (probs * (dprobs - delta[..., None])).astype(jnp.bfloat16)
    return (keys, probs, dscores)


def query_grads(kv_all, queries, grad_out, logsum, delta, width, factor):
    total_rows = kv_all.shape[1]
    size = math.gcd(total_rows, 512)

    def query_one_block(index, accum):
        block = lax.dynamic_slice_in_dim(kv_all, index * size, size, 1)
        keys, probs, dscores = block_grads(block, queries, grad_out, logsum, delta, width, factor)
        return accum + factor * jnp.einsum(
            "shqk,skhd->sqhd", dscores, keys, preferred_element_type=jnp.float32
        )

    return lax.fori_loop(
        0, total_rows // size, query_one_block, jnp.zeros(queries.shape, jnp.float32)
    )


def key_grads(kv_all, queries, grad_out, logsum, delta, width, factor, count):
    size = math.gcd(count, 512)
    seqs = queries.shape[0]

    def key_one_block(index, accum):
        block = lax.dynamic_slice_in_dim(kv_all, index * size, size, 1)
        keys, probs, dscores = block_grads(block, queries, grad_out, logsum, delta, width, factor)
        grad_vals = jnp.einsum(
            "shqk,sqhd->skhd",
            probs.astype(jnp.bfloat16),
            grad_out,
            preferred_element_type=jnp.float32,
        )
        grad_keys = factor * jnp.einsum(
            "shqk,sqhd->skhd", dscores, queries, preferred_element_type=jnp.float32
        )
        joined = jnp.concatenate(
            [grad_keys.reshape(seqs, size, width), grad_vals.reshape(seqs, size, width)], axis=-1
        )
        return lax.dynamic_update_slice_in_dim(
            accum, jnp.transpose(joined, (1, 0, 2)), index * size, 0
        )

    initial = jnp.zeros((count, seqs, 2 * width), jnp.float32)
    return lax.fori_loop(0, count // size, key_one_block, initial)


def adam_step(weight, grad, first, second, rate, decay_rate):
    new_first = BETA_ONE * first + (1.0 - BETA_ONE) * grad
    new_second = BETA_TWO * second + (1.0 - BETA_TWO) * grad * grad
    fixed_first = new_first / (1.0 - BETA_ONE**STEP)
    fixed_second = new_second / (1.0 - BETA_TWO**STEP)
    new_weight = weight - rate * (
        fixed_first / (jnp.sqrt(fixed_second) + ADAM_EPS) + decay_rate * weight
    )
    return (new_first, new_second, new_weight)


def mod_back(grad_hidden, ln_values, normed, scale_part, gain):
    grad_shift = jnp.sum(grad_hidden, axis=1)
    grad_scale = jnp.sum(grad_hidden * ln_values, axis=1)
    grad_ln = grad_hidden * (1.0 + scale_part)
    grad_gain = jnp.sum(grad_ln * normed, axis=(0, 1))
    return (grad_shift, grad_scale, grad_gain, grad_ln * gain)


def plain(
    tokens_in,
    cotangent,
    timesteps,
    span_start,
    span_len,
    vectors,
    w_ada,
    w_qkv,
    w_attn,
    w_in,
    w_out,
    m_vec,
    v_vec,
    m_ada,
    v_ada,
    m_qkv,
    v_qkv,
    m_attn,
    v_attn,
    m_in,
    v_in,
    m_out,
    v_out,
):
    seqs, group, width = tokens_in.shape
    heads = width // HD
    factor = HD ** (-0.5)
    flat_rows = seqs * group
    full_ada, full_qkv, full_attn, full_in, full_out = (
        lax.all_gather(w_ada.astype(jnp.bfloat16), ("dp", "seq"), axis=1, tiled=True),
        lax.all_gather(w_qkv.astype(jnp.bfloat16), ("dp", "seq"), axis=0, tiled=True),
        lax.all_gather(w_attn.astype(jnp.bfloat16), ("dp", "seq"), axis=0, tiled=True),
        lax.all_gather(w_in.astype(jnp.bfloat16), ("dp", "seq"), axis=0, tiled=True),
        lax.all_gather(w_out.astype(jnp.bfloat16), ("dp", "seq"), axis=0, tiled=True),
    )
    positions = lax.axis_index("seq") * group + jnp.arange(group, dtype=jnp.int32)
    masked = (positions[None, :] >= span_start[:, None]) & (
        positions[None, :] < (span_start + span_len)[:, None]
    )
    cond_bf = cond_input(timesteps).astype(jnp.bfloat16)
    modulation = jnp.dot(cond_bf, full_ada, preferred_element_type=jnp.float32) + vectors[
        2:8
    ].reshape(1, 6 * width)
    pieces = [modulation[:, which * width : (which + 1) * width][:, None, :] for which in range(6)]
    shift_one, scale_one, gate_one, shift_two, scale_two, gate_two = pieces
    start_tokens = jnp.where(
        masked[..., None], vectors[8][None, None, :], tokens_in.astype(jnp.float32)
    )
    normed_one, inv_one = normalize(start_tokens)
    ln_one = normed_one * vectors[0]
    hidden_one = (
        (ln_one * (1.0 + scale_one) + shift_one).astype(jnp.bfloat16).reshape(flat_rows, width)
    )
    projected = jnp.dot(hidden_one, full_qkv, preferred_element_type=jnp.float32).reshape(
        seqs, group, 3 * width
    )
    cosines, sines = rotary_tables(positions)
    queries = rotate(projected[..., :width].reshape(seqs, group, heads, HD), cosines, sines).astype(
        jnp.bfloat16
    )
    keys_here = rotate(
        projected[..., width : 2 * width].reshape(seqs, group, heads, HD), cosines, sines
    ).astype(jnp.bfloat16)
    values_here = projected[..., 2 * width :].astype(jnp.bfloat16)
    kv_local = jnp.concatenate([keys_here.reshape(seqs, group, width), values_here], axis=-1)
    initial = (
        jnp.full((seqs, heads, group), -1e30, jnp.float32),
        jnp.zeros((seqs, heads, group), jnp.float32),
        jnp.zeros((seqs, heads, group, HD), jnp.float32),
    )
    running, denom, accum = attend_piece(
        initial, lax.all_gather(kv_local, "seq", axis=1, tiled=True), queries, width, factor
    )
    attn_heads = accum / denom[..., None]
    logsum = running + jnp.log(denom)
    attn_rows = jnp.transpose(attn_heads, (0, 2, 1, 3)).reshape(flat_rows, width)
    attn_bf = attn_rows.astype(jnp.bfloat16)
    branch_one = jnp.dot(attn_bf, full_attn, preferred_element_type=jnp.float32).reshape(
        seqs, group, width
    )
    mid_tokens = start_tokens + gate_one * branch_one
    normed_two, inv_two = normalize(mid_tokens)
    ln_two = normed_two * vectors[1]
    hidden_two = (
        (ln_two * (1.0 + scale_two) + shift_two).astype(jnp.bfloat16).reshape(flat_rows, width)
    )
    pre_act = jnp.dot(hidden_two, full_in, preferred_element_type=jnp.float32)
    activ, gelu_back = jax.vjp(partial(jax.nn.gelu, approximate=True), pre_act)
    activ_bf = activ.astype(jnp.bfloat16)
    branch_two = jnp.dot(activ_bf, full_out, preferred_element_type=jnp.float32).reshape(
        seqs, group, width
    )
    block_out = (mid_tokens + gate_two * branch_two).astype(jnp.bfloat16)
    grad_y = cotangent.astype(jnp.float32)
    grad_gate_two = jnp.sum(grad_y * branch_two, axis=1)
    grad_branch_two = (grad_y * gate_two).astype(jnp.bfloat16).reshape(flat_rows, width)
    grad_w_out = jnp.dot(activ_bf.T, grad_branch_two, preferred_element_type=jnp.float32)
    grad_activ = jnp.dot(grad_branch_two, full_out.T, preferred_element_type=jnp.float32)
    grad_pre = gelu_back(grad_activ)[0].astype(jnp.bfloat16)
    grad_w_in = jnp.dot(hidden_two.T, grad_pre, preferred_element_type=jnp.float32)
    grad_hidden_two = jnp.dot(grad_pre, full_in.T, preferred_element_type=jnp.float32).reshape(
        seqs, group, width
    )
    grad_shift_two, grad_scale_two, grad_gain_two, grad_normed_two = mod_back(
        grad_hidden_two, ln_two, normed_two, scale_two, vectors[1]
    )
    grad_mid = grad_y + norm_back(normed_two, inv_two, grad_normed_two)
    grad_gate_one = jnp.sum(grad_mid * branch_one, axis=1)
    grad_branch_one = (grad_mid * gate_one).astype(jnp.bfloat16).reshape(flat_rows, width)
    grad_w_attn = jnp.dot(attn_bf.T, grad_branch_one, preferred_element_type=jnp.float32)
    grad_attn_bf = (
        jnp.dot(grad_branch_one, full_attn.T, preferred_element_type=jnp.float32)
        .astype(jnp.bfloat16)
        .reshape(seqs, group, heads, HD)
    )
    delta = jnp.einsum("sqhd,shqd->shq", grad_attn_bf.astype(jnp.float32), attn_heads)
    kv_all = lax.all_gather(kv_local, "seq", axis=1, tiled=True)
    grad_queries = query_grads(kv_all, queries, grad_attn_bf, logsum, delta, width, factor)
    grad_kv = jnp.transpose(
        lax.psum_scatter(
            key_grads(
                kv_all,
                queries,
                grad_attn_bf,
                logsum,
                delta,
                width,
                factor,
                group * lax.axis_size("seq"),
            ).astype(jnp.bfloat16),
            "seq",
            scatter_dimension=0,
            tiled=True,
        ).astype(jnp.float32),
        (1, 0, 2),
    )
    grad_keys = grad_kv[..., :width].reshape(seqs, group, heads, HD)
    grad_qkv = jnp.concatenate(
        [
            rotate_back(grad_queries, cosines, sines).reshape(seqs, group, width),
            rotate_back(grad_keys, cosines, sines).reshape(seqs, group, width),
            grad_kv[..., width:],
        ],
        axis=-1,
    )
    grad_qkv = grad_qkv.astype(jnp.bfloat16).reshape(flat_rows, 3 * width)
    grad_w_qkv = jnp.dot(hidden_one.T, grad_qkv, preferred_element_type=jnp.float32)
    grad_hidden_one = jnp.dot(grad_qkv, full_qkv.T, preferred_element_type=jnp.float32).reshape(
        seqs, group, width
    )
    grad_shift_one, grad_scale_one, grad_gain_one, grad_normed_one = mod_back(
        grad_hidden_one, ln_one, normed_one, scale_one, vectors[0]
    )
    grad_start = grad_mid + norm_back(normed_one, inv_one, grad_normed_one)
    grad_mask_row = jnp.sum(jnp.where(masked[..., None], grad_start, 0.0), axis=(0, 1))
    grad_input = jnp.where(masked[..., None], 0.0, grad_start)
    grad_mod = jnp.concatenate(
        [
            grad_shift_one,
            grad_scale_one,
            grad_gate_one,
            grad_shift_two,
            grad_scale_two,
            grad_gate_two,
        ],
        axis=1,
    )
    grad_w_ada = jnp.dot(cond_bf.astype(jnp.float32).T, grad_mod, precision=lax.Precision.HIGHEST)
    grad_vectors = jnp.concatenate(
        [
            grad_gain_one[None, :],
            grad_gain_two[None, :],
            jnp.sum(grad_mod, axis=0).reshape(6, width),
            grad_mask_row[None, :],
        ],
        axis=0,
    )
    red_ada, red_qkv, red_attn, red_in, red_out, red_vec = (
        lax.psum_scatter(grad_w_ada, ("dp", "seq"), scatter_dimension=1, tiled=True),
        lax.psum_scatter(grad_w_qkv, ("dp", "seq"), scatter_dimension=0, tiled=True),
        lax.psum_scatter(grad_w_attn, ("dp", "seq"), scatter_dimension=0, tiled=True),
        lax.psum_scatter(grad_w_in, ("dp", "seq"), scatter_dimension=0, tiled=True),
        lax.psum_scatter(grad_w_out, ("dp", "seq"), scatter_dimension=0, tiled=True),
        lax.psum_scatter(grad_vectors, ("dp", "seq"), scatter_dimension=1, tiled=True),
    )
    local_squares = jnp.float32(0.0)
    for reduced in (red_vec, red_ada, red_qkv, red_attn, red_in, red_out):
        local_squares = local_squares + jnp.sum(reduced * reduced)
    grad_norm = jnp.sqrt(lax.psum(local_squares, ("dp", "seq")))
    clip_factor = jnp.minimum(1.0, CLIP / (grad_norm + 1e-06))
    columns = red_vec.shape[1]
    own_vectors = lax.dynamic_slice_in_dim(
        vectors, lax.axis_index(("dp", "seq")) * columns, columns, 1
    )
    vec_out = adam_step(own_vectors, red_vec * clip_factor, m_vec, v_vec, RATE_VECTORS, 0.0)
    ada_out = adam_step(w_ada, red_ada * clip_factor, m_ada, v_ada, RATE, DECAY)
    qkv_out = adam_step(w_qkv, red_qkv * clip_factor, m_qkv, v_qkv, RATE, DECAY)
    attn_out = adam_step(w_attn, red_attn * clip_factor, m_attn, v_attn, RATE, DECAY)
    in_out = adam_step(w_in, red_in * clip_factor, m_in, v_in, RATE, DECAY)
    out_out = adam_step(w_out, red_out * clip_factor, m_out, v_out, RATE, DECAY)
    return (
        block_out,
        grad_input,
        grad_norm,
        vec_out[0],
        vec_out[1],
        vec_out[2],
        ada_out[0],
        ada_out[1],
        ada_out[2],
        qkv_out[0],
        qkv_out[1],
        qkv_out[2],
        attn_out[0],
        attn_out[1],
        attn_out[2],
        in_out[0],
        in_out[1],
        in_out[2],
        out_out[0],
        out_out[1],
        out_out[2],
    )


F32, BF = jnp.float32, jnp.bfloat16
MESH = pl.DeviceIdType.MESH
DP, LINE, SEQ, CHIPS, ALL = 4, 4, 8, 16, 32
ROWS, WIDTH, PACK = 128, 768, 640
HALF = WIDTH // 2
HALVES = ((0, 0), (0, 1), (0, 2), (2, 2), (1, 0), (1, 1), (1, 2), None, (2, 0), (2, 1))

def numbered(**counts):
    at = {}
    for name, count in counts.items():
        at[name] = sum(counts[other] for other in at)
    return SimpleNamespace(**at), sum(counts.values())


S, SEM_COUNT = numbered(
    load=11,
    cond=1,
    mix_qkv=1,
    mix_in=1,
    mix_attn=1,
    mod=1,
    w_qkv=1,
    w_attn=4,
    plane_in=1,
    w_in=4,
    w_out=4,
    group_qkv=4,
    group_attn=4,
    fw_qkv=1,
    fw_attn=1,
    fw_in=1,
    fw_out=1,
    tok=4,
    h2=4,
    dm=4,
    xf=4,
    o=1,
    mm=1,
    dh2=1,
    do=1,
    gp=1,
    dh1=5,
    pair_out=1,
    pair_in=1,
    pair_attn=1,
    pair_qkv=1,
    plane_attn=1,
    plane_qkv=1,
    line_out=5,
    line_in=5,
    slice_in=1,
    line_attn=1,
    line_qkv=1,
    last_in=1,
    last_attn=1,
    last_qkv=1,
    early=7,
    late=7,
    sq=1,
)

SCRATCH = dict(
    i_tok=((1, 128, 768), BF),
    i_cot=((1, 128, 768), BF),
    i_vec=((9, 768), F32),
    i_wada=((144, 128), F32),
    i_wqkv=((24, 2304), F32),
    i_wattn=((24, 768), F32),
    i_win=((24, 3072), F32),
    i_wout=((96, 768), F32),
    wide_qkv=((48, 3072), F32),
    wide_in=((48, 3072), F32),
    wide_attn=((48, 768), F32),
    s_qkv=((48, 3072), BF),
    s_in=((48, 3072), BF),
    s_attn=((48, 768), BF),
    w_qkv=((768, 768), BF),
    w_in=((4, 4, 48, 768), BF),
    w_attn=((768, 768), BF),
    w_out=((4, 2, 96, 768), BF),
    t_w_qkv=((640, 768), BF),
    t_w_attn=((768, 1024), BF),
    t_w_in=((768, 768), BF),
    t_w_out=((768, 768), BF),
    t_h1=((768, 512), BF),
    conds_all=((4, 8, 128), F32),
    mod_send=((4, 4, 128), F32),
    mod_got=((32, 4, 128), F32),
    mod_flat=((40, 128), F32),
    mod_pad=((8, 384), F32),
    turn=((2, 4, 128, 128), F32),
    dmod_flat=((4, 40, 128), F32),
    mod=((8, 768), F32),
    x0=((128, 768), F32),
    n1=((4, 128, 768), F32),
    inv1=((4, 128, 128), F32),
    x1=((128, 768), F32),
    n2=((128, 768), F32),
    inv2=((128, 128), F32),
    a=((128, 768), F32),
    dx1=((128, 768), F32),
    toks=((4, 128, 768), BF),
    h1=((4, 128, 768), BF),
    h2=((4, 128, 768), BF),
    dm=((4, 128, 768), BF),
    gb=((4, 128, 768), BF),
    du=((4, 128, 768), BF),
    xb=((2, 4, 128, 640), BF),
    pt=((3, 1024, 512), BF),
    vt=((2, 128, 1024), BF),
    kt=((2, 128, 1024), BF),
    back=((4, 128, 768), F32),
    ot=((2, 128, 512), F32),
    os=((4, 192, 128), BF),
    ob=((4, 192, 128), BF),
    o2=((4, 128, 128), BF),
    mms=((4, 128, 768), BF),
    mmr=((4, 128, 768), BF),
    dhs=((4, 128, 768), BF),
    dhr=((4, 128, 768), BF),
    das=((128, 768), BF),
    dos=((4, 192, 128), BF),
    dob=((4, 192, 128), BF),
    dst=((3, 1024, 512), BF),
    ga=((512, 640), F32),
    gps=((512, 512), BF),
    gpr=((512, 512), BF),
    dqkv=((4, 128, 768), BF),
    d1s=((4, 128, 768), BF),
    d1r=((4, 128, 768), BF),
    g_out=((4, 2, 96, 768), BF),
    g_in=((2, 4, 4, 48, 384), BF),
    g_attn=((2, 768, 384), BF),
    g_qkv=((2, 768, 384), BF),
    p_out=((4, 96, 768), BF),
    p_in=((4, 4, 48, 384), BF),
    p_attn=((768, 384), BF),
    p_qkv=((768, 384), BF),
    q_attn=((4, 192, 384), BF),
    q_qkv=((4, 192, 384), BF),
    m_attn=((192, 384), BF),
    m_qkv=((192, 384), BF),
    r_out=((4, 96, 768), BF),
    r_in=((4, 4, 48, 384), BF),
    via_in=((4, 48, 384), BF),
    via_out=((96, 768), BF),
    via_dh1=((128, 768), BF),
    m_in=((4, 48, 384), BF),
    u_in=((4, 48, 384), BF),
    r_attn=((4, 48, 384), BF),
    r_qkv=((4, 48, 384), BF),
    t_in=((4, 48, 384), F32),
    t_attn=((1, 48, 384), F32),
    t_qkv=((4, 48, 384), F32),
    f_in=((4, 2, 24, 384), F32),
    f_attn=((1, 2, 24, 384), F32),
    f_qkv=((4, 2, 24, 384), F32),
    early=((8, 768), F32),
    early_pair=((8, 768), F32),
    early_line=((4, 8, 384), F32),
    early_plane=((4, 8, 384), F32),
    early_all=((2, 4, 8, 384), F32),
    late=((4, 768), F32),
    late_pair=((4, 768), F32),
    late_line=((4, 4, 384), F32),
    late_plane=((4, 4, 384), F32),
    late_all=((2, 4, 4, 384), F32),
    sq=((32, 1, 128), F32),
)


def dot(left, right):
    return jnp.dot(left, right, preferred_element_type=F32)


def dot_nt(left, right):
    return lax.dot_general(left, right, (((1,), (1,)), ((), ())), preferred_element_type=F32)


def dot_tn(left, right):
    return lax.dot_general(left, right, (((0,), (0,)), ((), ())), preferred_element_type=F32)


def loop(count, body, start=0):
    def step(index, carry):
        body(index)
        return carry

    lax.fori_loop(start, count, step, 0)


def layer_kernel(
    i_time,
    i_start,
    i_len,
    h_tok,
    h_cot,
    h_vec,
    h_wada,
    h_wqkv,
    h_wattn,
    h_win,
    h_wout,
    o_y,
    o_dx,
    o_norm,
    o_gqkv,
    o_gattn,
    o_gin,
    o_gout,
    o_dmod,
    o_gvec,
    o_vec,
    o_conds,
    *scratch,
):
    r = SimpleNamespace(**dict(zip(SCRATCH, scratch)), when=scratch[-3])
    send_sems, recv_sems = scratch[-2:]
    i_tok, i_cot, i_vec, i_wada = r.i_tok, r.i_cot, r.i_vec, r.i_wada
    i_wqkv, i_wattn, i_win, i_wout = r.i_wqkv, r.i_wattn, r.i_win, r.i_wout
    b, s = lax.axis_index("dp"), lax.axis_index("seq")
    z, c = lax.div(s, 2), lax.rem(s, 2)
    mate = s + 1 - 2 * c
    chip = b * LINE + z
    me = b * SEQ + s
    drains = []

    def push(src, dst, at, to_b, to_s, out=None):
        pltpu.make_async_remote_copy(
            src_ref=src,
            dst_ref=dst,
            send_sem=send_sems.at[at if out is None else out],
            recv_sem=recv_sems.at[at],
            device_id=(to_b, to_s),
            device_id_type=MESH,
        ).start()

    def keep(src, dst, at):
        pltpu.make_async_copy(src, dst, recv_sems.at[at]).start()

    def got(at, like):
        pltpu.make_async_copy(like, like, recv_sems.at[at]).wait()

    def left(at, like):
        pltpu.make_async_copy(like, like, send_sems.at[at]).wait()

    def sent(at, like):
        drains.append(lambda: left(at, like))

    def by_core(body):
        for h, width in ((0, HALF), (1, PACK - HALF)):

            @pl.when(c == h)
            def _():
                body(slice(HALF * h, HALF * h + width), width)

    def sent_by_core(at, like):
        drains.append(lambda: by_core(lambda columns, width: left(at, like(width))))

    near = (b, b + 1 - 2 * lax.rem(b, 2), b + 2 - 4 * lax.div(b, 2), 3 - b)

    def toward(k):
        if k == 3:
            return 3, near[3]
        slot = 1 + c if k == 1 else 2 - c
        return slot, (1 - c) * near[k] + c * near[3 - k]

    def peers(body):
        for k in (1, 2, 3):
            body(*toward(k))

    def stack(body):
        for k in (1, 2, 3):
            body(lax.rem(z + k + 2 * c * (2 - k), LINE))

    def line_gather(block, at, near=True, rest=True):
        inner = 1 + lax.rem(z, 2)
        if near:
            push(block(z), block(z), at + z, b, 2 * inner + c, at)

        def one(to):
            relayed = ((z == 1) & (to == 3)) | ((z == 2) & (to == 0))

            @pl.when(jnp.logical_not(relayed | (to == inner)))
            def _():
                push(block(z), block(z), at + z, b, 2 * to + c, at)

        if rest:
            stack(one)

    def line_relay(block, at):
        for middle, source, to in ((2, 1, 3), (1, 2, 0)):

            @pl.when(z == middle)
            def _():
                got(at + source, block(source))
                push(block(source), block(source), at + source, b, 2 * to + c, at)

    def line_got(block, at, k):
        here = (k == z) | ((z == 2) & (k == 1)) | ((z == 1) & (k == 2))

        @pl.when(jnp.logical_not(here))
        def _():
            got(at + k, block(0))

    far = lax.div(z, 2)

    def line_order(j):
        return lax.rem(z + (2, 3 - 2 * far, 1 + 2 * far, 0)[j], LINE)

    def line_add(j, rows, dst, via, at):
        to = line_order(j)
        outer_chip = (z == 0) | (z == 3)

        def direct():
            push(rows(to), dst.at[z], at + z, b, 2 * to + c, at)

        if j == 0:

            @pl.when(outer_chip)
            def _():
                push(rows(to), via, at + 4, b, 2 * (1 + far) + c, at)

            @pl.when(jnp.logical_not(outer_chip))
            def _():
                direct()

        elif j < 3:
            direct()
        else:
            keep(rows(z), dst.at[z], at + z)

    def line_via(via, at, add):
        @pl.when((z == 1) | (z == 2))
        def _():
            got(at + 4, via)
            add()

    def line_done(dst, at):
        for k in range(4):
            missing = ((z == 1) & (k == 3)) | ((z == 2) & (k == 0))

            @pl.when(jnp.logical_not(missing))
            def _():
                got(at + k, dst.at[k])

    def line_clear(dst):
        for middle, k in ((1, 3), (2, 0)):

            @pl.when(z == middle)
            def _():
                dst[k] = jnp.zeros(dst.shape[1:], BF)

    lane = lax.broadcasted_iota(jnp.int32, (1, 128), 1)
    low = lane < 64
    own24 = pl.ds(pl.multiple_of(24 * c, 8), 24)
    mate24 = pl.ds(pl.multiple_of(24 * (1 - c), 8), 24)
    part = pl.ds(pl.multiple_of(HALF * c, 128), HALF)
    chip_rows = pl.ds(pl.multiple_of(48 * chip, 16), 48)
    group_rows = pl.ds(pl.multiple_of(192 * b, 16), 192)

    barrier = pltpu.get_barrier_semaphore()

    def greet(k):
        other = lax.rem(me + k, ALL)
        pl.semaphore_signal(
            barrier, inc=1, device_id=(lax.div(other, SEQ), lax.rem(other, SEQ)), device_id_type=MESH
        )

    loads = (
        (i_time, r.when.at[0]),
        (i_start, r.when.at[1]),
        (i_len, r.when.at[2]),
        (h_wqkv, i_wqkv),
        (h_win, i_win),
        (h_wattn, i_wattn),
        (h_wout, i_wout),
        (h_tok, i_tok),
        (h_vec, i_vec),
        (h_wada, i_wada),
        (h_cot, i_cot),
    )
    for k, (src, dst) in enumerate(loads):
        pltpu.make_async_copy(src, dst, recv_sems.at[S.load + k]).start()
    loop(ALL, greet, 1)
    for k, (src, dst) in enumerate(loads):
        pltpu.make_async_copy(src, dst, recv_sems.at[S.load + k]).wait()

    def natural(kind, p, head):
        return kind * WIDTH + 192 * p + 64 * head

    def half_at(ref, column, high):
        tile = ref[:, column // 128 * 128 : column // 128 * 128 + 128]
        return tile if (column % 128 == 64) == high else pltpu.roll(tile, 64, 1)

    for p in range(4):
        for tile in range(5):
            pair = []
            for high in (0, 1):
                which = HALVES[2 * tile + high]
                pair.append(
                    jnp.zeros((24, 128), F32)
                    if which is None
                    else half_at(i_wqkv, natural(which[0], p, which[1]), bool(high))
                )
            r.wide_qkv[own24, 768 * p + 128 * tile : 768 * p + 128 * tile + 128] = jnp.where(
                low, pair[0], pair[1]
            )
        r.wide_qkv[own24, 768 * p + 640 : 768 * p + 768] = jnp.zeros((24, 128), F32)
    r.wide_in[own24, :] = i_win[...]
    r.wide_attn[own24, :] = i_wattn[...]
    r.w_out[z, c] = i_wout[...].astype(BF)
    r.toks[z] = i_tok[0]
    line_clear(r.r_out)
    line_clear(r.r_in)
    line_clear(r.d1r)
    for ref in (r.q_qkv, r.r_qkv):
        ref[:, :, PACK - HALF : HALF] = jnp.zeros((4, ref.shape[1], WIDTH - PACK), BF)
    lanes8 = lax.broadcasted_iota(jnp.int32, (8, 128), 1)
    half_cond = COND // 2
    speed = jnp.exp((lanes8 % half_cond).astype(F32) * (-math.log(10000.0) / half_cond))
    angle = r.when[0, 0].astype(F32) * speed
    wave = jnp.where(lanes8 < half_cond, jnp.cos(angle), jnp.sin(angle))
    r.conds_all[b] = wave * (1.0 / (1.0 + jnp.exp(-wave)))
    pl.semaphore_wait(barrier, ALL - 1)

    def token_block(k):
        return r.toks.at[k]

    def attn_block(k):
        return r.w_attn.at[pl.ds(pl.multiple_of(192 * b + 48 * k, 16), 48), part]

    def in_block(k):
        return r.w_in.at[:, k, :, part]

    def out_block(k):
        return r.w_out.at[k, c]

    peers(lambda k, to: push(r.conds_all.at[b], r.conds_all.at[b], S.cond, to, s))
    sent(S.cond, r.conds_all.at[0:3])
    push(r.wide_qkv.at[own24], r.wide_qkv.at[own24], S.mix_qkv, b, mate)
    sent(S.mix_qkv, r.wide_qkv.at[0:24])
    push(r.wide_attn.at[own24], r.wide_attn.at[own24], S.mix_attn, b, mate)
    sent(S.mix_attn, r.wide_attn.at[0:24])
    push(r.wide_in.at[own24], r.wide_in.at[own24], S.mix_in, b, mate)
    sent(S.mix_in, r.wide_in.at[0:24])

    got(S.cond, r.conds_all.at[0:3])
    row8 = lax.broadcasted_iota(jnp.int32, (8, 128), 0)
    cond4 = jnp.zeros((8, 128), F32)
    for k in range(4):
        cond4 = jnp.where(row8 == k, r.conds_all[k], cond4)
    o_conds[...] = cond4
    wide = i_wada.shape[0]
    r.mod_pad[...] = jnp.zeros((8, 384), F32)
    r.mod_pad[:, 0:wide] = dot_nt(cond4.astype(BF), i_wada[...].astype(BF))
    columns = pltpu.roll(r.mod_pad[...], lax.rem(wide * me, 128), 1)
    for k in range(4):
        for t in range(3):
            r.mod_send[k, t : t + 1, :] = columns[k : k + 1, 128 * t : 128 * t + 128]
        r.mod_send[k, 3:4, :] = jnp.zeros((1, 128), F32)

    def send_mod(k):
        other = lax.rem(me + k, ALL)
        ob = lax.div(other, SEQ)
        push(r.mod_send.at[ob], r.mod_got.at[me], S.mod, ob, lax.rem(other, SEQ))

    loop(ALL, send_mod, 1)
    sent(S.mod, r.mod_got.at[0:31])
    keep(r.mod_send.at[b], r.mod_got.at[me], S.mod)

    def block(src, first):
        return src.at[:, pl.ds(pl.multiple_of(first, 128), HALF)]

    def slices_along_line():
        def send(columns, width):
            def rows(to):
                first = pl.multiple_of(WIDTH * to + columns.start, 128)
                return r.s_qkv.at[:, pl.ds(first, width)]

            dst = r.w_qkv.at[chip_rows, columns]
            stack(lambda to: push(rows(to), dst, S.w_qkv, b, 2 * to + c))
            keep(rows(z), dst, S.w_qkv)

        by_core(send)
        sent_by_core(S.w_qkv, lambda width: r.w_qkv.at[0:144, 0:width])

    def over_plane(dst, at):
        rows = dst.at[group_rows, part]
        peers(lambda k, to: push(rows, rows, at + k, to, s))
        for k in (1, 2, 3):
            sent(at + k, dst.at[0:192, 0:HALF])

    def share(dst, at, onward):
        for k in range(4):
            rows = dst.at[pl.ds(pl.multiple_of(192 * near[k], 16), 192), part]
            if k:
                got(at + k, rows)
            push(rows, rows, onward, b, mate)
        sent(onward, dst.at[:, 0:HALF])

    def line_share(block, at, onward):
        for k in range(4):
            line_got(block, at, k)
            push(block(k), block(k), onward, b, mate)

    got(S.mix_qkv, r.wide_qkv.at[0:24])
    r.s_qkv[...] = r.wide_qkv[...].astype(BF)
    slices_along_line()
    line_gather(token_block, S.tok, rest=False)
    sent(S.tok, r.toks.at[0:3])
    got(S.mix_attn, r.wide_attn.at[0:24])
    r.s_attn[...] = r.wide_attn[...].astype(BF)

    def qkv_over_plane(columns, width):
        got(S.w_qkv, r.w_qkv.at[0:192, 0:width])
        rows = r.w_qkv.at[group_rows, columns]
        peers(lambda k, to: push(rows, rows, S.group_qkv + k, to, s))

    by_core(qkv_over_plane)
    for k in (1, 2, 3):
        sent_by_core(S.group_qkv + k, lambda width: r.w_qkv.at[0:192, 0:width])
    line_gather(token_block, S.tok, near=False)
    for h in range(2):

        @pl.when(c == h)
        def _():
            r.w_attn[chip_rows, 384 * h : 384 * h + 384] = r.s_attn[:, 384 * h : 384 * h + 384]

    line_gather(attn_block, S.w_attn)
    sent(S.w_attn, r.w_attn.at[0:144, 0:HALF])
    line_gather(out_block, S.w_out)
    sent(S.w_out, r.w_out.at[0:3, 0])
    got(S.mix_in, r.wide_in.at[0:24])
    r.s_in[...] = r.wide_in[...].astype(BF)
    peers(
        lambda k, to: push(
            block(r.s_in, WIDTH * to + HALF * c), r.w_in.at[b, z, :, part], S.plane_in, to, s
        )
    )
    keep(block(r.s_in, WIDTH * b + HALF * c), r.w_in.at[b, z, :, part], S.plane_in)
    sent(S.plane_in, r.w_in.at[0:3, 0, :, 0:HALF])

    def hidden_rows(k):
        place = (2 * k + c) * ROWS + lax.broadcasted_iota(jnp.int32, (ROWS, 1), 0)
        return (place >= r.when[1, 0]) & (place < r.when[1, 0] + r.when[2, 0])

    def first_norm(tokens, k):
        x0 = jnp.where(hidden_rows(k), i_vec[8:9, :], tokens.astype(F32))
        normed, inverse = normalize(x0)
        r.n1[k] = normed
        r.inv1[k] = jnp.broadcast_to(inverse, (ROWS, 128))
        return x0

    r.x0[...] = first_norm(i_tok[0], z)

    got(S.mod, r.mod_got)
    r.mod_flat[...] = jnp.zeros((40, 128), F32)
    for k in range(ALL):
        first = 9 * k // 8
        r.mod_flat[first : first + 3, :] += r.mod_got[k, 0:3, :]
    for k in range(6):
        row = jnp.concatenate(
            [r.mod_flat[6 * k + t : 6 * k + t + 1, :] for t in range(6)], axis=1
        )
        r.mod[k : k + 1, :] = row + i_vec[2 + k : 3 + k, :]

    def mod(k):
        return r.mod[k : k + 1, :]

    def vec(k):
        return i_vec[k : k + 1, :]

    r.h1[z] = (r.n1[z] * vec(0) * (1.0 + mod(1)) + mod(0)).astype(BF)
    r.dm[0] = (i_cot[0].astype(F32) * mod(5)).astype(BF)
    peers(lambda k, to: push(r.dm.at[0], r.dm.at[k], S.dm + k, to, s))
    for k in (1, 2, 3):
        sent(S.dm + k, r.dm.at[0])

    lanes = lax.broadcasted_iota(jnp.int32, (ROWS, 128), 1)
    first_half = lanes % HD < HD // 2
    speed = jnp.exp((lanes % (HD // 2)).astype(F32) * (-math.log(10000.0) / (HD // 2)))
    row = lax.broadcasted_iota(jnp.int32, (ROWS, 128), 0)

    def table(k):
        angle = ((2 * k + c) * ROWS + row).astype(F32) * speed
        r.turn[0, k] = jnp.cos(angle)
        sine = jnp.sin(angle)
        r.turn[1, k] = jnp.where(first_half, -sine, sine)

    loop(LINE, table)

    line_relay(token_block, S.tok)

    def qkv_share(columns, width):
        for k in range(4):
            rows = r.w_qkv.at[pl.ds(pl.multiple_of(192 * near[k], 16), 192), columns]
            if k:
                got(S.group_qkv + k, rows)
            push(rows, rows, S.fw_qkv, b, mate)

    by_core(qkv_share)
    sent_by_core(S.fw_qkv, lambda width: r.w_qkv.at[:, 0:width])
    by_core(lambda columns, width: got(S.fw_qkv, r.w_qkv.at[:, 0 : PACK - width]))
    for k in range(5):
        columns = slice(128 * k, 128 * k + 128)
        r.t_w_qkv[columns, :] = r.w_qkv[:, columns].T

    def turned(tile, sign, k):
        other = jnp.where(first_half, pltpu.roll(tile, 96, 1), pltpu.roll(tile, 32, 1))
        return tile * r.turn[0, k] + sign * (other * r.turn[1, k])

    def project(j):
        k = lax.rem(z + j, LINE)

        @pl.when(j > 0)
        def _():
            line_got(token_block, S.tok, k)
            first_norm(r.toks[k], k)
            r.h1[k] = (r.n1[k] * vec(0) * (1.0 + mod(1)) + mod(0)).astype(BF)

        x = dot(r.h1[k], r.w_qkv[:, 0:PACK])
        tiles = [x[:, 128 * t : 128 * t + 128] for t in range(5)]
        tiles[0] = turned(tiles[0], 1.0, k) * 0.125
        tiles[1] = jnp.where(low, turned(tiles[1], 1.0, k) * 0.125, tiles[1])
        tiles[2] = turned(tiles[2], 1.0, k)
        tiles[3] = turned(tiles[3], 1.0, k)
        for t in range(5):
            r.xb[0, k, :, 128 * t : 128 * t + 128] = tiles[t].astype(BF)
        push(r.xb.at[0, k], r.xb.at[1, k], S.xf + k, b, mate)

    loop(4, project)
    line_relay(attn_block, S.w_attn)
    for k in range(4):
        line_got(attn_block, S.w_attn, k)
    over_plane(r.w_attn, S.group_attn)
    for k in range(4):
        sent(S.xf + k, r.xb.at[0, 0])

    for k in range(6):
        columns = slice(128 * k, 128 * k + 128)
        r.t_h1[columns, :] = r.h1[:, :, columns].reshape(512, 128).T
    for k in range(4):
        got(S.xf + k, r.xb.at[0, 0])

    def tile_of(t):
        return r.xb[:, :, :, 128 * t : 128 * t + 128].reshape(1024, 128)

    heads = ((0, 2, 4, True, True), (0, 2, 4, False, False), (1, 3, 1, True, False))

    def queries(head, first, size):
        q_tile, _, _, q_low, _ = heads[head]
        q = r.xb[0, first : first + size, :, 128 * q_tile : 128 * q_tile + 128]
        return jnp.where(low if q_low else ~low, q.reshape(size * 128, 128), jnp.zeros((), BF))

    r.vt[0] = tile_of(4).T
    r.vt[1] = tile_of(1).T
    for half in range(2):
        at = slice(256 * half, 256 * half + 256)
        for head in range(3):
            scores = dot_nt(tile_of(heads[head][1]), queries(head, 2 * half, 2))
            weights = jnp.exp(scores - jnp.max(scores, axis=0, keepdims=True))
            weights = weights * (1.0 / jnp.sum(weights, axis=0, keepdims=True))
            weights = weights.astype(BF)
            r.pt[head, :, at] = weights
            out = dot(r.vt[head // 2], weights)
            if head == 0:
                r.ot[0, 0:64, at] = out[0:64]
            elif head == 1:
                r.ot[0, 64:128, at] = out[64:128]
            else:
                r.ot[1, 0:64, at] = out[64:128]
                r.ot[1, 64:128, at] = jnp.zeros((64, 256), F32)
        for k in (2 * half, 2 * half + 1):
            across = slice(128 * k, 128 * k + 128)
            r.os[k, 0:128, :] = r.ot[0, :, across].T.astype(BF)
            third = r.ot[1, 0:64, across]
            third = jnp.concatenate([third, pltpu.roll(third, 64, 1)], axis=0)
            r.os[k, 128:192, :] = third.T[0:64].astype(BF)
        for to in (2 * half, 2 * half + 1):

            @pl.when(z == to)
            def _():
                keep(r.os.at[to], r.ob.at[z], S.o)

            @pl.when(z != to)
            def _():
                push(r.os.at[to], r.ob.at[z], S.o, b, 2 * to + c)

        if half == 0:
            line_relay(out_block, S.w_out)

    sent(S.o, r.os.at[0:3])
    got(S.plane_in, r.w_in.at[:, 0, :, 0:HALF])
    line_gather(in_block, S.w_in)
    sent(S.w_in, r.w_in.at[0:3, :, :, 0:HALF])
    for k in range(2):
        r.kt[k] = tile_of(2 + k).T
    share(r.w_attn, S.group_attn, S.fw_attn)
    got(S.fw_attn, r.w_attn.at[:, 0:HALF])
    for p in range(4):
        first = 192 * p
        r.t_w_attn[:, 256 * p : 256 * p + 128] = r.w_attn[first : first + 128, :].T
        third = r.w_attn[first + 128 : first + 192, :]
        r.t_w_attn[:, 256 * p + 128 : 256 * p + 256] = jnp.concatenate(
            [third, jnp.zeros_like(third)], axis=0
        ).T
    got(S.o, r.ob)
    a = jnp.zeros((ROWS, WIDTH), F32)
    for p in range(4):
        third = r.ob[p, 128:192, :].astype(F32)
        third = jnp.concatenate([third, pltpu.roll(third, 64, 1)], axis=0)
        r.o2[p] = jnp.where(low, third, 0.0).astype(BF)
        a += dot(r.ob[p, 0:128, :], r.w_attn[192 * p : 192 * p + 128, :])
        a += dot(r.o2[p, :, 0:64], r.w_attn[192 * p + 128 : 192 * p + 192, :])
    r.a[...] = a
    x1 = r.x0[...] + mod(2) * a
    r.x1[...] = x1
    n2, inv2 = normalize(x1)
    r.n2[...] = n2
    r.inv2[...] = jnp.broadcast_to(inv2, (ROWS, 128))
    r.h2[0] = (n2 * vec(1) * (1.0 + mod(4)) + mod(3)).astype(BF)
    peers(lambda k, to: push(r.h2.at[0], r.h2.at[k], S.h2 + k, to, s))
    for k in (1, 2, 3):
        sent(S.h2 + k, r.h2.at[0])
    line_relay(in_block, S.w_in)
    line_share(out_block, S.w_out, S.fw_out)
    sent(S.fw_out, r.w_out.at[:, 0])
    got(S.fw_out, r.w_out.at[:, 0])

    for k in range(6):
        columns = slice(128 * k, 128 * k + 128)
        r.t_w_out[columns, :] = r.w_out[:, :, :, columns].reshape(WIDTH, 128).T

    def feed_back(k):
        @pl.when(k > 0)
        def _():
            got(S.dm + k, r.dm.at[0])

        r.back[k] = dot(r.dm[k], r.t_w_out[...])

    loop(4, feed_back)
    line_share(in_block, S.w_in, S.fw_in)
    sent(S.fw_in, r.w_in.at[:, :, :, 0:HALF])
    got(S.fw_in, r.w_in.at[:, :, :, 0:HALF])
    for k in range(6):
        columns = slice(128 * k, 128 * k + 128)
        r.t_w_in[columns, :] = r.w_in[:, :, :, columns].reshape(WIDTH, 128).T

    def feed(first, count):
        at = slice(first, first + count)
        size = count * ROWS
        u = dot(r.h2[at].reshape(size, WIDTH), r.w_in[...].reshape(WIDTH, WIDTH))
        slope = 0.7978845608028654
        cube = 0.044715
        t = jnp.tanh(slope * (u + cube * u * u * u))
        r.gb[at] = (0.5 * u * (1.0 + t)).astype(BF).reshape(count, ROWS, WIDTH)
        bend = 0.5 * (1.0 + t) + 0.5 * u * (1.0 - t * t) * (slope * (1.0 + 3.0 * cube * u * u))
        du = (r.back[at].reshape(size, WIDTH) * bend).astype(BF)
        r.du[at] = du.reshape(count, ROWS, WIDTH)
        r.dhs[at] = dot(du, r.t_w_in[...]).astype(BF).reshape(count, ROWS, WIDTH)

    feed(0, 1)
    for first, count in ((1, 2), (3, 1)):
        for k in range(first, first + count):
            got(S.h2 + k, r.h2.at[0])
        feed(first, count)
        for k in range(first, first + count):
            slot, to = toward(k)
            push(r.dhs.at[slot], r.dhr.at[slot], S.dh2, to, s)
    sent(S.dh2, r.dhs.at[0:3])
    def gather(own, others):
        total = own[0].astype(F32)
        for k in (1, 2, 3):
            total += others[k].astype(F32)
        return total

    for k in range(2):
        rows = slice(384 * k, 384 * k + 384)
        result = dot_tn(r.gb[:, :, rows].reshape(512, 384), r.dm[...].reshape(512, 768))
        r.g_out[2 * k : 2 * k + 2] = result.astype(BF).reshape(2, 2, 96, 768)
    push(r.g_out.at[:, 1 - c], r.p_out, S.pair_out, b, mate)
    sent(S.pair_out, r.p_out)

    def to_mate(grad, dst, at):
        push(grad.at[1 - c], dst, at, b, mate)
        sent(at, dst)

    def pair_sum(grad, pair, at):
        got(at, pair)
        grad[c] = (grad[c].astype(F32) + pair[...].astype(F32)).astype(BF)

    def plane_sum(grad, dst, at, packed=False):
        def send(columns, width):
            def rows(to):
                return grad.at[c, pl.ds(pl.multiple_of(192 * to, 16), 192), 0:width]

            peers(lambda k, to: push(rows(to), dst.at[k, :, 0:width], at, to, s))
            keep(rows(b), dst.at[0, :, 0:width], at)

        if packed:
            by_core(send)
            sent_by_core(at, lambda width: dst.at[0:3, :, 0:width])
        else:
            send(None, HALF)
            sent(at, dst.at[0:3])

    def line_sum(src, total, dst, first, at, packed=False):
        def send(columns, width):
            got(first, src.at[:, :, 0:width])
            total[...] = (
                (src[0].astype(F32) + src[1].astype(F32))
                + (src[2].astype(F32) + src[3].astype(F32))
            ).astype(BF)

            def rows(to):
                return total.at[pl.ds(pl.multiple_of(48 * to, 16), 48), 0:width]

            stack(lambda to: push(rows(to), dst.at[z, :, 0:width], at, b, 2 * to + c))
            keep(rows(z), dst.at[z, :, 0:width], at)

        if packed:
            by_core(send)
            sent_by_core(at, lambda width: dst.at[0:3, :, 0:width])
        else:
            send(None, HALF)
            sent(at, dst.at[0:3])

    def trade(total, final, at):
        push(total.at[:, mate24], final.at[:, c], at, b, mate)
        sent(at, final.at[:, 0])
        final[:, c] = total[:, own24, :]

    def in_product(k):
        rows = slice(384 * k, 384 * k + 384)
        result = dot_tn(r.h2[:, :, rows].reshape(512, 384), r.du[...].reshape(512, 768)).astype(BF)
        for h in range(2):
            r.g_in[h, 2 * k : 2 * k + 2] = result[:, 384 * h : 384 * h + 384].reshape(2, 4, 48, 384)

    in_product(0)

    got(S.pair_out, r.p_out)
    for k in range(4):
        r.g_out[k, c] = (r.g_out[k, c].astype(F32) + r.p_out[k].astype(F32)).astype(BF)

    def out_rows(k):
        return r.g_out.at[k, c]

    for j in (0, 1):
        line_add(j, out_rows, r.r_out, r.via_out, S.line_out)
    in_product(1)
    to_mate(r.g_in, r.p_in, S.pair_in)

    def add_out():
        k = line_order(2)
        r.g_out[k, c] = (r.g_out[k, c].astype(F32) + r.via_out[...].astype(F32)).astype(BF)

    got(S.dh2, r.dhr.at[0:3])
    dh = gather(r.dhs, r.dhr)
    n2 = r.n2[...]
    inv2 = r.inv2[:, 0:1]
    r.early[...] = jnp.zeros((8, 768), F32)
    r.early[2:3, :] = jnp.sum(dh, axis=0, keepdims=True)
    both = jnp.sum(dh * n2, axis=0, keepdims=True)
    r.early[3:4, :] = both * vec(1)
    r.early[0:1, :] = both * (1.0 + mod(4))
    grad = dh * ((1.0 + mod(4)) * vec(1))
    dx1 = i_cot[0].astype(F32) + norm_back(n2, inv2, grad)
    r.dx1[...] = dx1
    r.early[1:2, :] = jnp.sum(dx1 * r.a[...], axis=0, keepdims=True)
    r.das[...] = (dx1 * mod(2)).astype(BF)
    for p in range(4):
        result = dot(r.das[...], r.t_w_attn[:, 256 * p : 256 * p + 256])
        r.dos[p, 0:128, :] = result[:, 0:128].astype(BF)
        third = result[:, 128:256]
        third = jnp.where(low, third[0:64], pltpu.roll(third[64:128], 64, 1))
        r.dos[p, 128:192, :] = third.astype(BF)
    stack(lambda to: push(r.dos.at[to], r.dob.at[z], S.do, b, 2 * to + c))
    keep(r.dos.at[z], r.dob.at[z], S.do)
    sent(S.do, r.dos.at[0:3])
    for t in range(3):
        at = slice(256 * t, 256 * t + 256)
        mm = dot(r.gb[...].reshape(512, WIDTH), r.w_out[:, :, :, at].reshape(WIDTH, 256))
        r.mms[:, :, at] = mm.astype(BF).reshape(4, ROWS, 256)
    peers(lambda k, to: push(r.mms.at[k], r.mmr.at[k], S.mm, to, s))
    sent(S.mm, r.mms.at[0:3])

    for p in range(4):
        for rows, left_side in (
            (slice(192 * p, 192 * p + 128), r.ob[p, 0:128, :]),
            (slice(192 * p + 128, 192 * p + 192), r.o2[p]),
        ):
            result = dot_tn(left_side, r.das[...])[0 : rows.stop - rows.start].astype(BF)
            r.g_attn[0, rows, :] = result[:, 0:HALF]
            r.g_attn[1, rows, :] = result[:, HALF:WIDTH]
    to_mate(r.g_attn, r.p_attn, S.pair_attn)

    def small_sum(src, pair, line, plane, whole, at):
        def first():
            push(src, pair, at, b, mate)
            sent(at, src)

        def second():
            got(at, pair)
            total = src[...] + pair[...]
            line[z] = (1 - c) * total[:, 0:HALF] + c * total[:, HALF:WIDTH]
            stack(lambda to: push(line.at[z], line.at[z], at + 1, b, 2 * to + c))
            sent(at + 1, line.at[0:3])

        def third():
            got(at + 1, line.at[0:3])
            plane[b] = (line[0] + line[1]) + (line[2] + line[3])
            peers(lambda k, to: push(plane.at[b], plane.at[b], at + 2, to, s))
            sent(at + 2, plane.at[0:3])

        def fourth():
            got(at + 2, plane.at[0:3])
            whole[c] = plane[...]
            push(plane, whole.at[c], at + 3, b, mate)
            sent(at + 3, plane)

        def rows(k):
            return jnp.concatenate([whole[0, k], whole[1, k]], axis=1)

        return first, second, third, fourth, rows

    early_steps = small_sum(
        r.early, r.early_pair, r.early_line, r.early_plane, r.early_all, S.early
    )
    late_steps = small_sum(r.late, r.late_pair, r.late_line, r.late_plane, r.late_all, S.late)

    pair_sum(r.g_in, r.p_in, S.pair_in)
    line_via(r.via_out, S.line_out, add_out)
    for j in (2, 3):
        line_add(j, out_rows, r.r_out, r.via_out, S.line_out)
    sent(S.line_out, r.r_out.at[0:3])

    def in_rows(k):
        return r.g_in.at[c, :, k]

    for j in (0, 1):
        line_add(j, in_rows, r.r_in, r.via_in, S.line_in)

    def add_in():
        k = line_order(2)
        r.g_in[c, :, k] = (r.g_in[c, :, k].astype(F32) + r.via_in[...].astype(F32)).astype(BF)

    pair_sum(r.g_attn, r.p_attn, S.pair_attn)
    plane_sum(r.g_attn, r.q_attn, S.plane_attn)

    got(S.do, r.dob)
    dot0 = r.dob[:, 0:128, :].reshape(512, 128)
    third = r.dob[:, 128:192, :].astype(F32).reshape(256, 128)
    other_rows = jnp.where(low, pltpu.roll(third, 64, 1), 0.0).reshape(4, 64, 128)
    third = jnp.where(low, third, 0.0).reshape(4, 64, 128)
    dot1 = jnp.concatenate([third, other_rows], axis=1).reshape(512, 128)
    zero = jnp.zeros((), BF)
    moved = pltpu.roll(dot1, 64, 1).astype(BF)
    grads = (jnp.where(low, dot0, zero), jnp.where(low, zero, dot0), moved)
    product = dot0.astype(F32).T * r.ot[0]
    deltas = (
        jnp.sum(product[0:64], axis=0, keepdims=True),
        jnp.sum(product[64:128], axis=0, keepdims=True),
        jnp.sum(dot1.T * r.ot[1], axis=0, keepdims=True),
    )
    for head in range(3):
        values = tile_of(heads[head][2])
        for half in range(2):
            at = slice(256 * half, 256 * half + 256)
            dp = dot_nt(values, grads[head][at])
            r.dst[head, :, at] = (
                r.pt[head, :, at].astype(F32) * (dp - deltas[head][:, at])
            ).astype(BF)

    def key_grads(rows):
        dk = [dot(r.dst[head, rows, :], queries(head, 0, 4)) for head in range(3)]
        dv = [dot(r.pt[head, rows, :], grads[head]) for head in range(3)]
        return (dv[2], dk[0] + dk[1], dk[2], dv[0] + dv[1])

    line_via(r.via_in, S.line_in, add_in)
    for j in (2, 3):
        line_add(j, in_rows, r.r_in, r.via_in, S.line_in)
    sent(S.line_in, r.r_in.at[0:3])
    for t, tile in enumerate(key_grads(slice(512, 1024))):
        r.gps[:, 128 * t : 128 * t + 128] = tile.astype(BF)
    push(r.gps, r.gpr, S.gp, b, mate)
    sent(S.gp, r.gps)
    for t, tile in enumerate(key_grads(slice(0, 512))):
        r.ga[:, 128 * t + 128 : 128 * t + 256] = tile
    for half in range(2):
        at = slice(256 * half, 256 * half + 256)
        turned_q = [dot(r.kt[head // 2], r.dst[head, :, at]) for head in range(3)]
        top = jnp.concatenate([turned_q[0][0:64], turned_q[1][64:128]], axis=0)
        r.ga[at, 0:128] = top.T * 0.125
        r.ga[at, 128:256] += turned_q[2].T * 0.125
    got(S.gp, r.gpr)

    def dh1_rows(k):
        return r.d1s.at[k]

    def back_turn(k):
        rows = pl.ds(pl.multiple_of(128 * k, 128), 128)
        tiles = [r.ga[rows, 0:128]] + [
            r.ga[rows, 128 * t : 128 * t + 128]
            + r.gpr[rows, 128 * t - 128 : 128 * t].astype(F32)
            for t in range(1, 5)
        ]
        tiles[0] = turned(tiles[0], -1.0, k)
        tiles[1] = jnp.where(low, turned(tiles[1], -1.0, k), tiles[1])
        tiles[2] = turned(tiles[2], -1.0, k)
        tiles[3] = turned(tiles[3], -1.0, k)
        for t in range(5):
            r.dqkv[k, :, 128 * t : 128 * t + 128] = tiles[t].astype(BF)
        r.dqkv[k, :, PACK:WIDTH] = jnp.zeros((128, 128), BF)

    back_turn(line_order(0))

    def unproject(j):
        k = line_order(j)
        partial_sum = dot(r.dqkv[k, :, 0:PACK], r.t_w_qkv[...])
        r.d1s[k] = partial_sum.astype(BF)
        if j == 2:

            def add():
                r.d1s[k] = (partial_sum + r.via_dh1[...].astype(F32)).astype(BF)

            line_via(r.via_dh1, S.dh1, add)
        line_add(j, dh1_rows, r.d1r, r.via_dh1, S.dh1)
        n = r.n1[k]
        e = partial_sum * ((1.0 + mod(1)) * vec(0))
        weight = jnp.where(hidden_rows(k), r.inv1[k][:, 0:1], 0.0)
        centred = (
            e
            - jnp.mean(e, axis=-1, keepdims=True)
            - n * jnp.mean(e * n, axis=-1, keepdims=True)
        )
        r.late[0:1, :] += jnp.sum(partial_sum * n, axis=0, keepdims=True)
        r.late[1:2, :] += jnp.sum(partial_sum, axis=0, keepdims=True)
        r.late[3:4, :] += jnp.sum(weight * centred, axis=0, keepdims=True)

    r.late[...] = jnp.zeros((4, 768), F32)
    r.late[3:4, :] = jnp.sum(
        jnp.where(hidden_rows(z), r.dx1[...], 0.0), axis=0, keepdims=True
    )
    unproject(0)
    for j in (1, 2, 3):
        back_turn(line_order(j))

    def qkv_rows(k):
        rows = pl.ds(pl.multiple_of(128 * k, 128), 128)
        result = dot(r.t_h1[rows, :], r.dqkv[...].reshape(512, WIDTH)).astype(BF)
        r.g_qkv[0, rows, :] = result[:, 0:HALF]
        r.g_qkv[1, rows, :] = result[:, HALF:WIDTH]

    loop(6, qkv_rows)
    to_mate(r.g_qkv, r.p_qkv, S.pair_qkv)
    unproject(1)
    pair_sum(r.g_qkv, r.p_qkv, S.pair_qkv)
    plane_sum(r.g_qkv, r.q_qkv, S.plane_qkv, True)
    got(S.mm, r.mmr.at[0:3])
    mm = gather(r.mms, r.mmr)
    o_y[...] = (r.x1[...] + mod(5) * mm).astype(BF)
    r.early[4:5, :] = jnp.sum(i_cot[0].astype(F32) * mm, axis=0, keepdims=True)
    early_steps[0]()
    unproject(2)
    unproject(3)
    sent(S.dh1, r.d1s.at[0:3])
    both = r.late[0:1, :]
    r.late[2:3, :] = both * vec(0)
    r.late[0:1, :] = both * (1.0 + mod(1))
    late_steps[0]()
    early_steps[1]()
    line_sum(r.q_attn, r.m_attn, r.r_attn, S.plane_attn, S.line_attn)
    late_steps[1]()

    line_done(r.r_in, S.line_in)
    r.m_in[...] = (
        (r.r_in[0].astype(F32) + r.r_in[1].astype(F32))
        + (r.r_in[2].astype(F32) + r.r_in[3].astype(F32))
    ).astype(BF)
    peers(lambda k, to: push(r.m_in.at[to], r.u_in.at[b], S.slice_in, to, s))
    keep(r.m_in.at[b], r.u_in.at[b], S.slice_in)
    sent(S.slice_in, r.u_in.at[0:3])
    line_sum(r.q_qkv, r.m_qkv, r.r_qkv, S.plane_qkv, S.line_qkv, True)
    early_steps[2]()
    late_steps[2]()

    line_done(r.d1r, S.dh1)
    dh = (r.d1r[0].astype(F32) + r.d1r[1].astype(F32)) + (
        r.d1r[2].astype(F32) + r.d1r[3].astype(F32)
    )
    n1 = r.n1[z]
    grad = dh * ((1.0 + mod(1)) * vec(0))
    dx0 = r.dx1[...] + norm_back(n1, r.inv1[z][:, 0:1], grad)
    o_dx[...] = jnp.where(hidden_rows(z), 0.0, dx0)
    early_steps[3]()
    late_steps[3]()

    line_done(r.r_out, S.line_out)
    total = (r.r_out[0].astype(F32) + r.r_out[1].astype(F32)) + (
        r.r_out[2].astype(F32) + r.r_out[3].astype(F32)
    )
    o_gout[...] = total
    squares = total * total
    squares = jnp.sum(squares[:, 0:128] + squares[:, 128:256] + squares[:, 256:384]
                      + squares[:, 384:512] + squares[:, 512:640] + squares[:, 640:768],
                      axis=0, keepdims=True)

    def fold(value):
        total = value[:, 0:128] * value[:, 0:128]
        for t in range(1, value.shape[1] // 128):
            total += value[:, 128 * t : 128 * t + 128] * value[:, 128 * t : 128 * t + 128]
        return jnp.sum(total, axis=0, keepdims=True)

    got(S.slice_in, r.u_in)
    r.t_in[...] = r.u_in[...].astype(F32)
    for p in range(4):
        squares += fold(r.t_in[p])
    trade(r.t_in, r.f_in, S.last_in)
    got(S.line_attn, r.r_attn)
    r.t_attn[0] = (r.r_attn[0].astype(F32) + r.r_attn[1].astype(F32)) + (
        r.r_attn[2].astype(F32) + r.r_attn[3].astype(F32)
    )
    squares += fold(r.t_attn[0])
    trade(r.t_attn, r.f_attn, S.last_attn)
    by_core(lambda columns, width: got(S.line_qkv, r.r_qkv.at[:, :, 0:width]))
    r.t_qkv[...] = r.r_qkv[...].astype(F32)
    trade(r.t_qkv, r.f_qkv, S.last_qkv)
    for p in range(4):
        squares += fold(r.t_qkv[p])
    r.sq[me] = squares

    def send_sq(k):
        other = lax.rem(me + k, ALL)
        push(r.sq.at[me], r.sq.at[me], S.sq, lax.div(other, SEQ), lax.rem(other, SEQ))

    loop(ALL, send_sq, 1)
    sent(S.sq, r.sq.at[0:31])
    got(S.last_in, r.f_in.at[:, 0])
    got(S.last_attn, r.f_attn.at[:, 0])
    for h in range(2):
        for p in range(4):
            value = r.f_in[p, h]
            o_gin[:, 768 * p + 384 * h : 768 * p + 384 * h + 384] = value
        value = r.f_attn[0, h]
        o_gattn[:, 384 * h : 384 * h + 384] = value
    got(S.last_qkv, r.f_qkv.at[:, 0])
    where = {which: index for index, which in enumerate(HALVES) if which is not None}

    def packed_half(chunk, high):
        kind, rest = chunk // 12, chunk % 12
        index = where[(kind, rest % 3)]
        t = index // 2
        tile = r.f_qkv[rest // 3, t // 3, :, t % 3 * 128 : t % 3 * 128 + 128]
        return tile if index % 2 == high else pltpu.roll(tile, 64, 1)

    for t in range(18):
        o_gqkv[:, 128 * t : 128 * t + 128] = jnp.where(
            low, packed_half(2 * t, 0), packed_half(2 * t + 1, 1)
        )
    got(S.early + 3, r.early_all.at[0])
    got(S.late + 3, r.late_all.at[0])
    early_rows = [early_steps[4](k) for k in range(4)]
    late_rows = [late_steps[4](k) for k in range(4)]
    mods = []
    for k in range(4):
        early, late = early_rows[k], late_rows[k]
        rows = jnp.concatenate([late[1:3], early[1:5], jnp.zeros((2, 768), F32)], axis=0)
        for n in range(6):
            for m in range(6):
                r.dmod_flat[k, 6 * n + m : 6 * n + m + 1, :] = rows[
                    n : n + 1, 128 * m : 128 * m + 128
                ]
        mods.append(rows)
    gain = jnp.concatenate(
        [
            sum(late_rows[k][0:1] for k in range(4)),
            sum(early_rows[k][0:1] for k in range(4)),
            (mods[0] + mods[1] + mods[2] + mods[3])[0:6],
        ],
        axis=0,
    )
    mask_row = sum(late_rows[k][3:4] for k in range(4))
    gains = jnp.concatenate([gain, mask_row, jnp.zeros((7, 768), F32)], axis=0)
    masters = jnp.concatenate([i_vec[...], jnp.zeros((7, 768), F32)], axis=0)
    own = lax.rem(WIDTH - 24 * me, WIDTH)
    o_gvec[...] = pltpu.roll(gains, own, 1)[:, 0:128]
    o_vec[...] = pltpu.roll(masters, own, 1)[:, 0:128]
    r.mod_pad[...] = jnp.zeros((8, 384), F32)
    window = lax.div(wide * me, 128)
    for k in range(4):
        rows = r.dmod_flat[k, pl.ds(window, 3), :]
        for m in range(3):
            r.mod_pad[k : k + 1, 128 * m : 128 * m + 128] = rows[m : m + 1, :]
    o_dmod[...] = pltpu.roll(r.mod_pad[...], lax.rem(384 - lax.rem(wide * me, 128), 384), 1)[:, 0:256]
    small = jnp.sum(gain * gain) + jnp.sum(mask_row * mask_row)
    conds = [r.conds_all[k][0:1].astype(BF).astype(F32) for k in range(4)]
    for k in range(4):
        for m in range(k, 4):
            term = jnp.sum(mods[k] * mods[m]) * jnp.sum(conds[k] * conds[m])
            small += term if m == k else 2.0 * term
    got(S.sq, r.sq.at[0:31])
    total = r.sq[0]
    for k in range(1, ALL):
        total += r.sq[k]
    o_norm[...] = jnp.broadcast_to(jnp.sqrt(jnp.sum(total) + small), (8, 128))

    for drained in drains:
        drained()


def run_layer(*args):
    shapes = (
        ((ROWS, WIDTH), BF),
        ((ROWS, WIDTH), F32),
        ((8, 128), F32),
        ((24, 3 * WIDTH), F32),
        ((24, WIDTH), F32),
        ((24, 4 * WIDTH), F32),
        ((96, WIDTH), F32),
        ((8, 256), F32),
        ((16, 128), F32),
        ((16, 128), F32),
        ((8, 128), F32),
    )
    whole = pl.BlockSpec(memory_space=pltpu.VMEM)
    return pl.pallas_call(
        layer_kernel,
        out_shape=[jax.ShapeDtypeStruct(shape, kind) for shape, kind in shapes],
        in_specs=[pl.BlockSpec(memory_space=pl.ANY)] * len(args),
        out_specs=[whole] * len(shapes),
        scratch_shapes=[pltpu.VMEM(shape, kind) for shape, kind in SCRATCH.values()]
        + [pltpu.SMEM((3, 1), jnp.int32)]
        + [pltpu.SemaphoreType.DMA((SEM_COUNT,)), pltpu.SemaphoreType.DMA((SEM_COUNT,))],
        compiler_params=pltpu.CompilerParams(
            collective_id=0, has_side_effects=True, vmem_limit_bytes=60 * 1024 * 1024
        ),
    )(*args)


HELD = (2, 8, 9, 7, 10, 3, 4, 5, 6)


def finish_kernel(*refs):
    sources, outs, refs = refs[:28], refs[28:49], refs[49:]
    near, results, load_sems, store_sems = refs[:28], refs[28:46], refs[46], refs[47]
    norm, g_vec, own_vec, dmod, conds = near[:5]
    weights, moments = (own_vec, *near[9:14]), near[14:26]

    order = list(range(5)) + [14, 15, 9, 16, 17]
    for k in range(2, 6):
        order += [3 + k, 8 + k, 14 + 2 * k, 15 + 2 * k]
    loads = {}
    for n in order:
        source = sources[HELD[n]] if n < 9 else sources[n + 2]
        loads[n] = pltpu.make_async_copy(source, near[n], load_sems.at[n])
        loads[n].start()
    for n in (26, 27):
        loads[n] = pltpu.make_async_copy(sources[n - 26], near[n], load_sems.at[n])
        loads[n].start()
    for n in order[:10]:
        loads[n].wait()
    outs[2][0, 0] = norm[0, 0]
    clip = jnp.minimum(1.0, CLIP / (norm[0:1, 0:1] + 1e-06))
    wide, narrow = near[9].shape[0], moments[0].shape[1]
    rounded = conds[...].astype(BF).astype(F32)
    turned_mod = dmod[...].T
    g_ada = turned_mod[0:wide, 0:1] * rounded[0:1, :]
    for k in range(1, 4):
        g_ada += turned_mod[0:wide, k : k + 1] * rounded[k : k + 1, :]
    stores = []
    for k in range(6):
        if k > 1:
            for n in order[2 + 4 * k : 6 + 4 * k]:
                loads[n].wait()
        grad = g_vec[0:9, 0:narrow] if k == 0 else g_ada if k == 1 else near[3 + k][...]
        updated = adam_step(
            weights[k][...] if k else own_vec[0:9, 0:narrow],
            grad * clip,
            moments[2 * k][...],
            moments[2 * k + 1][...],
            RATE if k else RATE_VECTORS,
            DECAY if k else 0.0,
        )
        for n in range(3):
            at = 3 * k + n
            results[at][...] = updated[n]
            stores.append(pltpu.make_async_copy(results[at], outs[3 + at], store_sems.at[at]))
            stores[-1].start()
    for n in (26, 27):
        loads[n].wait()
        stores.append(pltpu.make_async_copy(near[n], outs[n - 26].at[0], store_sems.at[n - 8]))
        stores[-1].start()
    for copy in stores:
        copy.wait()


def run_finish(partial_results, weights, moments):
    shapes = [((1, ROWS, WIDTH), BF), ((1, ROWS, WIDTH), F32), ((1, 1), F32)]
    for moment in moments[::2]:
        shapes += [(moment.shape, F32)] * 3
    far = pl.BlockSpec(memory_space=pl.ANY)
    specs = [far] * len(shapes)
    specs[2] = pl.BlockSpec(memory_space=pltpu.SMEM)
    near = [partial_results[k] for k in HELD] + [*weights, *moments, *partial_results[:2]]
    args = (*partial_results, *weights, *moments)
    return pl.pallas_call(
        finish_kernel,
        out_shape=[jax.ShapeDtypeStruct(shape, kind) for shape, kind in shapes],
        in_specs=[far] * len(args),
        out_specs=specs,
        scratch_shapes=[pltpu.VMEM(array.shape, array.dtype) for array in near]
        + [pltpu.VMEM(shape, kind) for shape, kind in shapes[3:]]
        + [pltpu.SemaphoreType.DMA((28,)), pltpu.SemaphoreType.DMA((20,))],
        compiler_params=pltpu.CompilerParams(vmem_limit_bytes=60 * 1024 * 1024),
    )(*args)


def slices(
    tokens_in,
    cotangent,
    timesteps,
    span_start,
    span_len,
    vectors,
    w_ada,
    w_qkv,
    w_attn,
    w_in,
    w_out,
    m_vec,
    v_vec,
    m_ada,
    v_ada,
    m_qkv,
    v_qkv,
    m_attn,
    v_attn,
    m_in,
    v_in,
    m_out,
    v_out,
):
    partial_results = run_layer(
        timesteps,
        span_start,
        span_len,
        tokens_in,
        cotangent,
        vectors,
        w_ada.T,
        w_qkv,
        w_attn,
        w_in,
        w_out,
    )
    moments = (
        m_vec,
        v_vec,
        m_ada.T,
        v_ada.T,
        m_qkv,
        v_qkv,
        m_attn,
        v_attn,
        m_in,
        v_in,
        m_out,
        v_out,
    )
    results = run_finish(partial_results, (w_ada.T, w_qkv, w_attn, w_in, w_out), moments)
    ada_results = [result.T for result in results[6:9]]
    return (*results[:2], results[2].reshape(()), *results[3:6], *ada_results, *results[9:])


def solution(mesh):
    in_specs = (
        P("dp", "seq", None),
        P("dp", "seq", None),
        P("dp"),
        P("dp"),
        P("dp"),
        P(),
        P(None, ("dp", "seq")),
        P(("dp", "seq"), None),
        P(("dp", "seq"), None),
        P(("dp", "seq"), None),
        P(("dp", "seq"), None),
        P(None, ("dp", "seq")),
        P(None, ("dp", "seq")),
        P(None, ("dp", "seq")),
        P(None, ("dp", "seq")),
        P(("dp", "seq"), None),
        P(("dp", "seq"), None),
        P(("dp", "seq"), None),
        P(("dp", "seq"), None),
        P(("dp", "seq"), None),
        P(("dp", "seq"), None),
        P(("dp", "seq"), None),
        P(("dp", "seq"), None),
    )
    out_specs = (
        P("dp", "seq", None),
        P("dp", "seq", None),
        P(),
        P(None, ("dp", "seq")),
        P(None, ("dp", "seq")),
        P(None, ("dp", "seq")),
        P(None, ("dp", "seq")),
        P(None, ("dp", "seq")),
        P(None, ("dp", "seq")),
        P(("dp", "seq"), None),
        P(("dp", "seq"), None),
        P(("dp", "seq"), None),
        P(("dp", "seq"), None),
        P(("dp", "seq"), None),
        P(("dp", "seq"), None),
        P(("dp", "seq"), None),
        P(("dp", "seq"), None),
        P(("dp", "seq"), None),
        P(("dp", "seq"), None),
        P(("dp", "seq"), None),
        P(("dp", "seq"), None),
    )
    sizes = dict(mesh.shape)
    local = slices if (sizes["dp"], sizes["seq"]) == (4, 8) else plain
    return jax.shard_map(local, mesh=mesh, in_specs=in_specs, out_specs=out_specs, check_vma=False)
```

```python
from functools import partial
import math
from types import SimpleNamespace

import jax
import jax.numpy as jnp
from jax import lax
from jax.experimental import pallas as pl
from jax.experimental.pallas import tpu as pltpu
from jax.sharding import PartitionSpec as P

HD = 64
COND = 128
STEP = 10


BETA_ONE = 0.9
BETA_TWO = 0.999
ADAM_EPS = 1e-08
RATE = 0.1
RATE_VECTORS = 0.3
DECAY = 0.01
CLIP = 1.0
NORM_EPS = 1e-05


def cond_input(timesteps):
    half_cond = COND // 2
    freqs = jnp.exp(jnp.arange(half_cond, dtype=jnp.float32) * (-math.log(10000.0) / half_cond))
    angles = timesteps.astype(jnp.float32)[:, None] * freqs[None, :]
    return jax.nn.silu(jnp.concatenate([jnp.cos(angles), jnp.sin(angles)], axis=1))


def rotary_tables(positions):
    half_head = HD // 2
    inverse = jnp.exp(jnp.arange(half_head, dtype=jnp.float32) * (-math.log(10000.0) / half_head))
    angles = positions.astype(jnp.float32)[:, None] * inverse[None, :]
    return (jnp.cos(angles), jnp.sin(angles))


def rotate(values, cosines, sines):
    half_head = values.shape[-1] // 2
    first = values[..., :half_head]
    second = values[..., half_head:]
    cos_b = cosines[:, None, :]
    sin_b = sines[:, None, :]
    return jnp.concatenate(
        [first * cos_b - second * sin_b, second * cos_b + first * sin_b], axis=-1
    )


def rotate_back(grads, cosines, sines):
    half_head = grads.shape[-1] // 2
    first = grads[..., :half_head]
    second = grads[..., half_head:]
    cos_b = cosines[:, None, :]
    sin_b = sines[:, None, :]
    return jnp.concatenate(
        [first * cos_b + second * sin_b, second * cos_b - first * sin_b], axis=-1
    )


def normalize(values):
    centre = jnp.mean(values, axis=-1, keepdims=True)
    centred = values - centre
    inverse = lax.rsqrt(jnp.mean(centred * centred, axis=-1, keepdims=True) + NORM_EPS)
    return (centred * inverse, inverse)


def norm_back(normed, inverse, grad):
    return inverse * (
        grad
        - jnp.mean(grad, axis=-1, keepdims=True)
        - normed * jnp.mean(grad * normed, axis=-1, keepdims=True)
    )


def split_kv(block, width):
    seqs, block_rows = (block.shape[0], block.shape[1])
    keys = block[..., :width].reshape(seqs, block_rows, width // HD, HD)
    values = block[..., width:].reshape(seqs, block_rows, width // HD, HD)
    return (keys, values)


def attend_piece(carry, piece, queries, width, factor):
    piece_rows = piece.shape[1]
    size = math.gcd(piece_rows, 512)

    def attend_one_block(index, state):
        running, denom, accum = state
        block = lax.dynamic_slice_in_dim(piece, index * size, size, 1)
        keys, values = split_kv(block, width)
        scores = (
            jnp.einsum("sqhd,skhd->shqk", queries, keys, preferred_element_type=jnp.float32)
            * factor
        )
        highest = jnp.maximum(running, jnp.max(scores, axis=-1))
        shrink = jnp.exp(running - highest)
        weights = jnp.exp(scores - highest[..., None])
        denom = denom * shrink + jnp.sum(weights, axis=-1)
        accum = accum * shrink[..., None] + jnp.einsum(
            "shqk,skhd->shqd",
            weights.astype(jnp.bfloat16),
            values,
            preferred_element_type=jnp.float32,
        )
        return (highest, denom, accum)

    return lax.fori_loop(0, piece_rows // size, attend_one_block, carry)


def block_grads(block, queries, grad_out, logsum, delta, width, factor):
    keys, values = split_kv(block, width)
    scores = (
        jnp.einsum("sqhd,skhd->shqk", queries, keys, preferred_element_type=jnp.float32) * factor
    )
    probs = jnp.exp(scores - logsum[..., None])
    dprobs = jnp.einsum("sqhd,skhd->shqk", grad_out, values, preferred_element_type=jnp.float32)
    dscores = (probs * (dprobs - delta[..., None])).astype(jnp.bfloat16)
    return (keys, probs, dscores)


def query_grads(kv_all, queries, grad_out, logsum, delta, width, factor):
    total_rows = kv_all.shape[1]
    size = math.gcd(total_rows, 512)

    def query_one_block(index, accum):
        block = lax.dynamic_slice_in_dim(kv_all, index * size, size, 1)
        keys, probs, dscores = block_grads(block, queries, grad_out, logsum, delta, width, factor)
        return accum + factor * jnp.einsum(
            "shqk,skhd->sqhd", dscores, keys, preferred_element_type=jnp.float32
        )

    return lax.fori_loop(
        0, total_rows // size, query_one_block, jnp.zeros(queries.shape, jnp.float32)
    )


def key_grads(kv_all, queries, grad_out, logsum, delta, width, factor, count):
    size = math.gcd(count, 512)
    seqs = queries.shape[0]

    def key_one_block(index, accum):
        block = lax.dynamic_slice_in_dim(kv_all, index * size, size, 1)
        keys, probs, dscores = block_grads(block, queries, grad_out, logsum, delta, width, factor)
        grad_vals = jnp.einsum(
            "shqk,sqhd->skhd",
            probs.astype(jnp.bfloat16),
            grad_out,
            preferred_element_type=jnp.float32,
        )
        grad_keys = factor * jnp.einsum(
            "shqk,sqhd->skhd", dscores, queries, preferred_element_type=jnp.float32
        )
        joined = jnp.concatenate(
            [grad_keys.reshape(seqs, size, width), grad_vals.reshape(seqs, size, width)], axis=-1
        )
        return lax.dynamic_update_slice_in_dim(
            accum, jnp.transpose(joined, (1, 0, 2)), index * size, 0
        )

    initial = jnp.zeros((count, seqs, 2 * width), jnp.float32)
    return lax.fori_loop(0, count // size, key_one_block, initial)


def adam_step(weight, grad, first, second, rate, decay_rate):
    new_first = BETA_ONE * first + (1.0 - BETA_ONE) * grad
    new_second = BETA_TWO * second + (1.0 - BETA_TWO) * grad * grad
    fixed_first = new_first / (1.0 - BETA_ONE**STEP)
    fixed_second = new_second / (1.0 - BETA_TWO**STEP)
    new_weight = weight - rate * (
        fixed_first / (jnp.sqrt(fixed_second) + ADAM_EPS) + decay_rate * weight
    )
    return (new_first, new_second, new_weight)


def mod_back(grad_hidden, ln_values, normed, scale_part, gain):
    grad_shift = jnp.sum(grad_hidden, axis=1)
    grad_scale = jnp.sum(grad_hidden * ln_values, axis=1)
    grad_ln = grad_hidden * (1.0 + scale_part)
    grad_gain = jnp.sum(grad_ln * normed, axis=(0, 1))
    return (grad_shift, grad_scale, grad_gain, grad_ln * gain)


def plain(
    tokens_in,
    cotangent,
    timesteps,
    span_start,
    span_len,
    vectors,
    w_ada,
    w_qkv,
    w_attn,
    w_in,
    w_out,
    m_vec,
    v_vec,
    m_ada,
    v_ada,
    m_qkv,
    v_qkv,
    m_attn,
    v_attn,
    m_in,
    v_in,
    m_out,
    v_out,
):
    seqs, group, width = tokens_in.shape
    heads = width // HD
    factor = HD ** (-0.5)
    flat_rows = seqs * group
    full_ada, full_qkv, full_attn, full_in, full_out = (
        lax.all_gather(w_ada.astype(jnp.bfloat16), ("dp", "seq"), axis=1, tiled=True),
        lax.all_gather(w_qkv.astype(jnp.bfloat16), ("dp", "seq"), axis=0, tiled=True),
        lax.all_gather(w_attn.astype(jnp.bfloat16), ("dp", "seq"), axis=0, tiled=True),
        lax.all_gather(w_in.astype(jnp.bfloat16), ("dp", "seq"), axis=0, tiled=True),
        lax.all_gather(w_out.astype(jnp.bfloat16), ("dp", "seq"), axis=0, tiled=True),
    )
    positions = lax.axis_index("seq") * group + jnp.arange(group, dtype=jnp.int32)
    masked = (positions[None, :] >= span_start[:, None]) & (
        positions[None, :] < (span_start + span_len)[:, None]
    )
    cond_bf = cond_input(timesteps).astype(jnp.bfloat16)
    modulation = jnp.dot(cond_bf, full_ada, preferred_element_type=jnp.float32) + vectors[
        2:8
    ].reshape(1, 6 * width)
    pieces = [modulation[:, which * width : (which + 1) * width][:, None, :] for which in range(6)]
    shift_one, scale_one, gate_one, shift_two, scale_two, gate_two = pieces
    start_tokens = jnp.where(
        masked[..., None], vectors[8][None, None, :], tokens_in.astype(jnp.float32)
    )
    normed_one, inv_one = normalize(start_tokens)
    ln_one = normed_one * vectors[0]
    hidden_one = (
        (ln_one * (1.0 + scale_one) + shift_one).astype(jnp.bfloat16).reshape(flat_rows, width)
    )
    projected = jnp.dot(hidden_one, full_qkv, preferred_element_type=jnp.float32).reshape(
        seqs, group, 3 * width
    )
    cosines, sines = rotary_tables(positions)
    queries = rotate(projected[..., :width].reshape(seqs, group, heads, HD), cosines, sines).astype(
        jnp.bfloat16
    )
    keys_here = rotate(
        projected[..., width : 2 * width].reshape(seqs, group, heads, HD), cosines, sines
    ).astype(jnp.bfloat16)
    values_here = projected[..., 2 * width :].astype(jnp.bfloat16)
    kv_local = jnp.concatenate([keys_here.reshape(seqs, group, width), values_here], axis=-1)
    initial = (
        jnp.full((seqs, heads, group), -1e30, jnp.float32),
        jnp.zeros((seqs, heads, group), jnp.float32),
        jnp.zeros((seqs, heads, group, HD), jnp.float32),
    )
    running, denom, accum = attend_piece(
        initial, lax.all_gather(kv_local, "seq", axis=1, tiled=True), queries, width, factor
    )
    attn_heads = accum / denom[..., None]
    logsum = running + jnp.log(denom)
    attn_rows = jnp.transpose(attn_heads, (0, 2, 1, 3)).reshape(flat_rows, width)
    attn_bf = attn_rows.astype(jnp.bfloat16)
    branch_one = jnp.dot(attn_bf, full_attn, preferred_element_type=jnp.float32).reshape(
        seqs, group, width
    )
    mid_tokens = start_tokens + gate_one * branch_one
    normed_two, inv_two = normalize(mid_tokens)
    ln_two = normed_two * vectors[1]
    hidden_two = (
        (ln_two * (1.0 + scale_two) + shift_two).astype(jnp.bfloat16).reshape(flat_rows, width)
    )
    pre_act = jnp.dot(hidden_two, full_in, preferred_element_type=jnp.float32)
    activ, gelu_back = jax.vjp(partial(jax.nn.gelu, approximate=True), pre_act)
    activ_bf = activ.astype(jnp.bfloat16)
    branch_two = jnp.dot(activ_bf, full_out, preferred_element_type=jnp.float32).reshape(
        seqs, group, width
    )
    block_out = (mid_tokens + gate_two * branch_two).astype(jnp.bfloat16)
    grad_y = cotangent.astype(jnp.float32)
    grad_gate_two = jnp.sum(grad_y * branch_two, axis=1)
    grad_branch_two = (grad_y * gate_two).astype(jnp.bfloat16).reshape(flat_rows, width)
    grad_w_out = jnp.dot(activ_bf.T, grad_branch_two, preferred_element_type=jnp.float32)
    grad_activ = jnp.dot(grad_branch_two, full_out.T, preferred_element_type=jnp.float32)
    grad_pre = gelu_back(grad_activ)[0].astype(jnp.bfloat16)
    grad_w_in = jnp.dot(hidden_two.T, grad_pre, preferred_element_type=jnp.float32)
    grad_hidden_two = jnp.dot(grad_pre, full_in.T, preferred_element_type=jnp.float32).reshape(
        seqs, group, width
    )
    grad_shift_two, grad_scale_two, grad_gain_two, grad_normed_two = mod_back(
        grad_hidden_two, ln_two, normed_two, scale_two, vectors[1]
    )
    grad_mid = grad_y + norm_back(normed_two, inv_two, grad_normed_two)
    grad_gate_one = jnp.sum(grad_mid * branch_one, axis=1)
    grad_branch_one = (grad_mid * gate_one).astype(jnp.bfloat16).reshape(flat_rows, width)
    grad_w_attn = jnp.dot(attn_bf.T, grad_branch_one, preferred_element_type=jnp.float32)
    grad_attn_bf = (
        jnp.dot(grad_branch_one, full_attn.T, preferred_element_type=jnp.float32)
        .astype(jnp.bfloat16)
        .reshape(seqs, group, heads, HD)
    )
    delta = jnp.einsum("sqhd,shqd->shq", grad_attn_bf.astype(jnp.float32), attn_heads)
    kv_all = lax.all_gather(kv_local, "seq", axis=1, tiled=True)
    grad_queries = query_grads(kv_all, queries, grad_attn_bf, logsum, delta, width, factor)
    grad_kv = jnp.transpose(
        lax.psum_scatter(
            key_grads(
                kv_all,
                queries,
                grad_attn_bf,
                logsum,
                delta,
                width,
                factor,
                group * lax.axis_size("seq"),
            ).astype(jnp.bfloat16),
            "seq",
            scatter_dimension=0,
            tiled=True,
        ).astype(jnp.float32),
        (1, 0, 2),
    )
    grad_keys = grad_kv[..., :width].reshape(seqs, group, heads, HD)
    grad_qkv = jnp.concatenate(
        [
            rotate_back(grad_queries, cosines, sines).reshape(seqs, group, width),
            rotate_back(grad_keys, cosines, sines).reshape(seqs, group, width),
            grad_kv[..., width:],
        ],
        axis=-1,
    )
    grad_qkv = grad_qkv.astype(jnp.bfloat16).reshape(flat_rows, 3 * width)
    grad_w_qkv = jnp.dot(hidden_one.T, grad_qkv, preferred_element_type=jnp.float32)
    grad_hidden_one = jnp.dot(grad_qkv, full_qkv.T, preferred_element_type=jnp.float32).reshape(
        seqs, group, width
    )
    grad_shift_one, grad_scale_one, grad_gain_one, grad_normed_one = mod_back(
        grad_hidden_one, ln_one, normed_one, scale_one, vectors[0]
    )
    grad_start = grad_mid + norm_back(normed_one, inv_one, grad_normed_one)
    grad_mask_row = jnp.sum(jnp.where(masked[..., None], grad_start, 0.0), axis=(0, 1))
    grad_input = jnp.where(masked[..., None], 0.0, grad_start)
    grad_mod = jnp.concatenate(
        [
            grad_shift_one,
            grad_scale_one,
            grad_gate_one,
            grad_shift_two,
            grad_scale_two,
            grad_gate_two,
        ],
        axis=1,
    )
    grad_w_ada = jnp.dot(cond_bf.astype(jnp.float32).T, grad_mod, precision=lax.Precision.HIGHEST)
    grad_vectors = jnp.concatenate(
        [
            grad_gain_one[None, :],
            grad_gain_two[None, :],
            jnp.sum(grad_mod, axis=0).reshape(6, width),
            grad_mask_row[None, :],
        ],
        axis=0,
    )
    red_ada, red_qkv, red_attn, red_in, red_out, red_vec = (
        lax.psum_scatter(grad_w_ada, ("dp", "seq"), scatter_dimension=1, tiled=True),
        lax.psum_scatter(grad_w_qkv, ("dp", "seq"), scatter_dimension=0, tiled=True),
        lax.psum_scatter(grad_w_attn, ("dp", "seq"), scatter_dimension=0, tiled=True),
        lax.psum_scatter(grad_w_in, ("dp", "seq"), scatter_dimension=0, tiled=True),
        lax.psum_scatter(grad_w_out, ("dp", "seq"), scatter_dimension=0, tiled=True),
        lax.psum_scatter(grad_vectors, ("dp", "seq"), scatter_dimension=1, tiled=True),
    )
    local_squares = jnp.float32(0.0)
    for reduced in (red_vec, red_ada, red_qkv, red_attn, red_in, red_out):
        local_squares = local_squares + jnp.sum(reduced * reduced)
    grad_norm = jnp.sqrt(lax.psum(local_squares, ("dp", "seq")))
    clip_factor = jnp.minimum(1.0, CLIP / (grad_norm + 1e-06))
    columns = red_vec.shape[1]
    own_vectors = lax.dynamic_slice_in_dim(
        vectors, lax.axis_index(("dp", "seq")) * columns, columns, 1
    )
    vec_out = adam_step(own_vectors, red_vec * clip_factor, m_vec, v_vec, RATE_VECTORS, 0.0)
    ada_out = adam_step(w_ada, red_ada * clip_factor, m_ada, v_ada, RATE, DECAY)
    qkv_out = adam_step(w_qkv, red_qkv * clip_factor, m_qkv, v_qkv, RATE, DECAY)
    attn_out = adam_step(w_attn, red_attn * clip_factor, m_attn, v_attn, RATE, DECAY)
    in_out = adam_step(w_in, red_in * clip_factor, m_in, v_in, RATE, DECAY)
    out_out = adam_step(w_out, red_out * clip_factor, m_out, v_out, RATE, DECAY)
    return (
        block_out,
        grad_input,
        grad_norm,
        vec_out[0],
        vec_out[1],
        vec_out[2],
        ada_out[0],
        ada_out[1],
        ada_out[2],
        qkv_out[0],
        qkv_out[1],
        qkv_out[2],
        attn_out[0],
        attn_out[1],
        attn_out[2],
        in_out[0],
        in_out[1],
        in_out[2],
        out_out[0],
        out_out[1],
        out_out[2],
    )


F32, BF = jnp.float32, jnp.bfloat16
MESH = pl.DeviceIdType.MESH
DP, LINE, SEQ, CHIPS, ALL = 4, 4, 8, 16, 32
ROWS, WIDTH, PACK = 128, 768, 640
HALF = WIDTH // 2
HALVES = ((0, 0), (0, 1), (0, 2), (2, 2), (1, 0), (1, 1), (1, 2), None, (2, 0), (2, 1))

def numbered(**counts):
    at = {}
    for name, count in counts.items():
        at[name] = sum(counts[other] for other in at)
    return SimpleNamespace(**at), sum(counts.values())


S, SEM_COUNT = numbered(
    load=11,
    cond=1,
    mix_qkv=1,
    mix_in=1,
    mix_attn=1,
    mod=1,
    w_qkv=1,
    w_attn=4,
    plane_in=1,
    w_in=4,
    w_out=4,
    group_qkv=4,
    group_attn=4,
    fw_qkv=1,
    fw_attn=1,
    fw_in=1,
    fw_out=1,
    tok=4,
    h2=4,
    dm=4,
    xf=4,
    o=1,
    mm=1,
    dh2=1,
    do=1,
    gp=1,
    dh1=5,
    pair_out=1,
    pair_in=1,
    pair_attn=1,
    pair_qkv=1,
    plane_attn=1,
    plane_qkv=1,
    line_out=5,
    line_in=5,
    slice_in=1,
    line_attn=1,
    line_qkv=1,
    last_in=1,
    last_attn=1,
    last_qkv=1,
    early=7,
    late=7,
    sq=1,
)

SCRATCH = dict(
    i_tok=((1, 128, 768), BF),
    i_cot=((1, 128, 768), BF),
    i_vec=((9, 768), F32),
    i_wada=((144, 128), F32),
    i_wqkv=((24, 2304), F32),
    i_wattn=((24, 768), F32),
    i_win=((24, 3072), F32),
    i_wout=((96, 768), F32),
    wide_qkv=((48, 3072), F32),
    wide_in=((48, 3072), F32),
    wide_attn=((48, 768), F32),
    s_qkv=((48, 3072), BF),
    s_in=((48, 3072), BF),
    s_attn=((48, 768), BF),
    w_qkv=((768, 768), BF),
    w_in=((4, 4, 48, 768), BF),
    w_attn=((768, 768), BF),
    w_out=((4, 2, 96, 768), BF),
    t_w_qkv=((640, 768), BF),
    t_w_attn=((768, 1024), BF),
    t_h1=((768, 512), BF),
    conds_all=((4, 8, 128), F32),
    mod_send=((4, 4, 128), F32),
    mod_got=((32, 4, 128), F32),
    mod_flat=((40, 128), F32),
    mod_pad=((8, 384), F32),
    turn=((2, 4, 128, 128), F32),
    dmod_flat=((4, 40, 128), F32),
    mod=((8, 768), F32),
    x0=((128, 768), F32),
    n1=((4, 128, 768), F32),
    inv1=((4, 128, 128), F32),
    x1=((128, 768), F32),
    n2=((128, 768), F32),
    inv2=((128, 128), F32),
    a=((128, 768), F32),
    dx1=((128, 768), F32),
    toks=((4, 128, 768), BF),
    h1=((4, 128, 768), BF),
    h2=((4, 128, 768), BF),
    dm=((4, 128, 768), BF),
    gb=((4, 128, 768), BF),
    du=((4, 128, 768), BF),
    xb=((2, 4, 128, 640), BF),
    pt=((3, 1024, 512), BF),
    vt=((2, 128, 1024), BF),
    kt=((2, 128, 1024), BF),
    back=((4, 128, 768), F32),
    ot=((2, 128, 512), F32),
    os=((4, 192, 128), BF),
    ob=((4, 192, 128), BF),
    o2=((4, 128, 128), BF),
    mms=((4, 128, 768), BF),
    mmr=((4, 128, 768), BF),
    dhs=((4, 128, 768), BF),
    dhr=((4, 128, 768), BF),
    das=((128, 768), BF),
    dos=((4, 192, 128), BF),
    dob=((4, 192, 128), BF),
    dst=((3, 1024, 512), BF),
    ga=((512, 640), F32),
    gps=((512, 512), BF),
    gpr=((512, 512), BF),
    dqkv=((4, 128, 768), BF),
    d1s=((4, 128, 768), BF),
    d1r=((4, 128, 768), BF),
    g_out=((4, 2, 96, 768), BF),
    g_in=((2, 4, 4, 48, 384), BF),
    g_attn=((2, 768, 384), BF),
    g_qkv=((2, 768, 384), BF),
    p_out=((4, 96, 768), BF),
    p_in=((4, 4, 48, 384), BF),
    p_attn=((768, 384), BF),
    p_qkv=((768, 384), BF),
    q_attn=((4, 192, 384), BF),
    q_qkv=((4, 192, 384), BF),
    m_attn=((192, 384), BF),
    m_qkv=((192, 384), BF),
    r_out=((4, 96, 768), BF),
    r_in=((4, 4, 48, 384), BF),
    via_in=((4, 48, 384), BF),
    via_out=((96, 768), BF),
    via_dh1=((128, 768), BF),
    m_in=((4, 48, 384), BF),
    u_in=((4, 48, 384), BF),
    r_attn=((4, 48, 384), BF),
    r_qkv=((4, 48, 384), BF),
    t_in=((4, 48, 384), F32),
    t_attn=((1, 48, 384), F32),
    t_qkv=((4, 48, 384), F32),
    f_in=((4, 2, 24, 384), F32),
    f_attn=((1, 2, 24, 384), F32),
    f_qkv=((4, 2, 24, 384), F32),
    early=((8, 768), F32),
    early_pair=((8, 768), F32),
    early_line=((4, 8, 384), F32),
    early_plane=((4, 8, 384), F32),
    early_all=((2, 4, 8, 384), F32),
    late=((4, 768), F32),
    late_pair=((4, 768), F32),
    late_line=((4, 4, 384), F32),
    late_plane=((4, 4, 384), F32),
    late_all=((2, 4, 4, 384), F32),
    sq=((32, 1, 128), F32),
)


def dot(left, right):
    return jnp.dot(left, right, preferred_element_type=F32)


def dot_nt(left, right):
    return lax.dot_general(left, right, (((1,), (1,)), ((), ())), preferred_element_type=F32)


def dot_tn(left, right):
    return lax.dot_general(left, right, (((0,), (0,)), ((), ())), preferred_element_type=F32)


def loop(count, body, start=0):
    def step(index, carry):
        body(index)
        return carry

    lax.fori_loop(start, count, step, 0)


def layer_kernel(
    i_time,
    i_start,
    i_len,
    h_tok,
    h_cot,
    h_vec,
    h_wada,
    h_wqkv,
    h_wattn,
    h_win,
    h_wout,
    o_y,
    o_dx,
    o_norm,
    o_gqkv,
    o_gattn,
    o_gin,
    o_gout,
    o_dmod,
    o_gvec,
    o_vec,
    o_conds,
    *scratch,
):
    r = SimpleNamespace(**dict(zip(SCRATCH, scratch)), when=scratch[-3])
    send_sems, recv_sems = scratch[-2:]
    i_tok, i_cot, i_vec, i_wada = r.i_tok, r.i_cot, r.i_vec, r.i_wada
    i_wqkv, i_wattn, i_win, i_wout = r.i_wqkv, r.i_wattn, r.i_win, r.i_wout
    b, s = lax.axis_index("dp"), lax.axis_index("seq")
    z, c = lax.div(s, 2), lax.rem(s, 2)
    mate = s + 1 - 2 * c
    chip = b * LINE + z
    me = b * SEQ + s
    drains = []

    def push(src, dst, at, to_b, to_s, out=None):
        pltpu.make_async_remote_copy(
            src_ref=src,
            dst_ref=dst,
            send_sem=send_sems.at[at if out is None else out],
            recv_sem=recv_sems.at[at],
            device_id=(to_b, to_s),
            device_id_type=MESH,
        ).start()

    def keep(src, dst, at):
        pltpu.make_async_copy(src, dst, recv_sems.at[at]).start()

    def got(at, like):
        pltpu.make_async_copy(like, like, recv_sems.at[at]).wait()

    def left(at, like):
        pltpu.make_async_copy(like, like, send_sems.at[at]).wait()

    def sent(at, like):
        drains.append(lambda: left(at, like))

    def by_core(body):
        for h, width in ((0, HALF), (1, PACK - HALF)):

            @pl.when(c == h)
            def _():
                body(slice(HALF * h, HALF * h + width), width)

    def sent_by_core(at, like):
        drains.append(lambda: by_core(lambda columns, width: left(at, like(width))))

    near = (b, b + 1 - 2 * lax.rem(b, 2), b + 2 - 4 * lax.div(b, 2), 3 - b)

    def toward(k):
        if k == 3:
            return 3, near[3]
        slot = 1 + c if k == 1 else 2 - c
        return slot, (1 - c) * near[k] + c * near[3 - k]

    def peers(body):
        for k in (1, 2, 3):
            body(*toward(k))

    def stack(body):
        for k in (1, 2, 3):
            body(lax.rem(z + k + 2 * c * (2 - k), LINE))

    def line_gather(block, at, near=True, rest=True):
        inner = 1 + lax.rem(z, 2)
        if near:
            push(block(z), block(z), at + z, b, 2 * inner + c, at)

        def one(to):
            relayed = ((z == 1) & (to == 3)) | ((z == 2) & (to == 0))

            @pl.when(jnp.logical_not(relayed | (to == inner)))
            def _():
                push(block(z), block(z), at + z, b, 2 * to + c, at)

        if rest:
            stack(one)

    def line_relay(block, at):
        for middle, source, to in ((2, 1, 3), (1, 2, 0)):

            @pl.when(z == middle)
            def _():
                got(at + source, block(source))
                push(block(source), block(source), at + source, b, 2 * to + c, at)

    def line_got(block, at, k):
        here = (k == z) | ((z == 2) & (k == 1)) | ((z == 1) & (k == 2))

        @pl.when(jnp.logical_not(here))
        def _():
            got(at + k, block(0))

    far = lax.div(z, 2)

    def line_order(j):
        return lax.rem(z + (2, 3 - 2 * far, 1 + 2 * far, 0)[j], LINE)

    def line_add(j, rows, dst, via, at):
        to = line_order(j)
        outer_chip = (z == 0) | (z == 3)

        def direct():
            push(rows(to), dst.at[z], at + z, b, 2 * to + c, at)

        if j == 0:

            @pl.when(outer_chip)
            def _():
                push(rows(to), via, at + 4, b, 2 * (1 + far) + c, at)

            @pl.when(jnp.logical_not(outer_chip))
            def _():
                direct()

        elif j < 3:
            direct()
        else:
            keep(rows(z), dst.at[z], at + z)

    def line_via(via, at, add):
        @pl.when((z == 1) | (z == 2))
        def _():
            got(at + 4, via)
            add()

    def line_done(dst, at):
        for k in range(4):
            missing = ((z == 1) & (k == 3)) | ((z == 2) & (k == 0))

            @pl.when(jnp.logical_not(missing))
            def _():
                got(at + k, dst.at[k])

    def line_clear(dst):
        for middle, k in ((1, 3), (2, 0)):

            @pl.when(z == middle)
            def _():
                dst[k] = jnp.zeros(dst.shape[1:], BF)

    lane = lax.broadcasted_iota(jnp.int32, (1, 128), 1)
    low = lane < 64
    own24 = pl.ds(pl.multiple_of(24 * c, 8), 24)
    mate24 = pl.ds(pl.multiple_of(24 * (1 - c), 8), 24)
    part = pl.ds(pl.multiple_of(HALF * c, 128), HALF)
    chip_rows = pl.ds(pl.multiple_of(48 * chip, 16), 48)
    group_rows = pl.ds(pl.multiple_of(192 * b, 16), 192)

    barrier = pltpu.get_barrier_semaphore()

    def greet(k):
        other = lax.rem(me + k, ALL)
        pl.semaphore_signal(
            barrier, inc=1, device_id=(lax.div(other, SEQ), lax.rem(other, SEQ)), device_id_type=MESH
        )

    loads = (
        (i_time, r.when.at[0]),
        (i_start, r.when.at[1]),
        (i_len, r.when.at[2]),
        (h_wqkv, i_wqkv),
        (h_win, i_win),
        (h_wattn, i_wattn),
        (h_wout, i_wout),
        (h_tok, i_tok),
        (h_vec, i_vec),
        (h_wada, i_wada),
        (h_cot, i_cot),
    )
    for k, (src, dst) in enumerate(loads):
        pltpu.make_async_copy(src, dst, recv_sems.at[S.load + k]).start()
    loop(ALL, greet, 1)
    for k, (src, dst) in enumerate(loads):
        pltpu.make_async_copy(src, dst, recv_sems.at[S.load + k]).wait()

    def natural(kind, p, head):
        return kind * WIDTH + 192 * p + 64 * head

    def half_at(ref, column, high):
        tile = ref[:, column // 128 * 128 : column // 128 * 128 + 128]
        return tile if (column % 128 == 64) == high else pltpu.roll(tile, 64, 1)

    for p in range(4):
        for tile in range(5):
            pair = []
            for high in (0, 1):
                which = HALVES[2 * tile + high]
                pair.append(
                    jnp.zeros((24, 128), F32)
                    if which is None
                    else half_at(i_wqkv, natural(which[0], p, which[1]), bool(high))
                )
            r.wide_qkv[own24, 768 * p + 128 * tile : 768 * p + 128 * tile + 128] = jnp.where(
                low, pair[0], pair[1]
            )
        r.wide_qkv[own24, 768 * p + 640 : 768 * p + 768] = jnp.zeros((24, 128), F32)
    r.wide_in[own24, :] = i_win[...]
    r.wide_attn[own24, :] = i_wattn[...]
    r.w_out[z, c] = i_wout[...].astype(BF)
    r.toks[z] = i_tok[0]
    line_clear(r.r_out)
    line_clear(r.r_in)
    line_clear(r.d1r)
    for ref in (r.q_qkv, r.r_qkv):
        ref[:, :, PACK - HALF : HALF] = jnp.zeros((4, ref.shape[1], WIDTH - PACK), BF)
    lanes8 = lax.broadcasted_iota(jnp.int32, (8, 128), 1)
    half_cond = COND // 2
    speed = jnp.exp((lanes8 % half_cond).astype(F32) * (-math.log(10000.0) / half_cond))
    angle = r.when[0, 0].astype(F32) * speed
    wave = jnp.where(lanes8 < half_cond, jnp.cos(angle), jnp.sin(angle))
    r.conds_all[b] = wave * (1.0 / (1.0 + jnp.exp(-wave)))
    pl.semaphore_wait(barrier, ALL - 1)

    def token_block(k):
        return r.toks.at[k]

    def attn_block(k):
        return r.w_attn.at[pl.ds(pl.multiple_of(192 * b + 48 * k, 16), 48), part]

    def in_block(k):
        return r.w_in.at[:, k, :, part]

    def out_block(k):
        return r.w_out.at[k, c]

    peers(lambda k, to: push(r.conds_all.at[b], r.conds_all.at[b], S.cond, to, s))
    sent(S.cond, r.conds_all.at[0:3])
    push(r.wide_qkv.at[own24], r.wide_qkv.at[own24], S.mix_qkv, b, mate)
    sent(S.mix_qkv, r.wide_qkv.at[0:24])
    push(r.wide_attn.at[own24], r.wide_attn.at[own24], S.mix_attn, b, mate)
    sent(S.mix_attn, r.wide_attn.at[0:24])
    push(r.wide_in.at[own24], r.wide_in.at[own24], S.mix_in, b, mate)
    sent(S.mix_in, r.wide_in.at[0:24])

    got(S.cond, r.conds_all.at[0:3])
    row8 = lax.broadcasted_iota(jnp.int32, (8, 128), 0)
    cond4 = jnp.zeros((8, 128), F32)
    for k in range(4):
        cond4 = jnp.where(row8 == k, r.conds_all[k], cond4)
    o_conds[...] = cond4
    wide = i_wada.shape[0]
    r.mod_pad[...] = jnp.zeros((8, 384), F32)
    r.mod_pad[:, 0:wide] = dot_nt(cond4.astype(BF), i_wada[...].astype(BF))
    columns = pltpu.roll(r.mod_pad[...], lax.rem(wide * me, 128), 1)
    for k in range(4):
        for t in range(3):
            r.mod_send[k, t : t + 1, :] = columns[k : k + 1, 128 * t : 128 * t + 128]
        r.mod_send[k, 3:4, :] = jnp.zeros((1, 128), F32)

    def send_mod(k):
        other = lax.rem(me + k, ALL)
        ob = lax.div(other, SEQ)
        push(r.mod_send.at[ob], r.mod_got.at[me], S.mod, ob, lax.rem(other, SEQ))

    loop(ALL, send_mod, 1)
    sent(S.mod, r.mod_got.at[0:31])
    keep(r.mod_send.at[b], r.mod_got.at[me], S.mod)

    def block(src, first):
        return src.at[:, pl.ds(pl.multiple_of(first, 128), HALF)]

    def slices_along_line():
        def send(columns, width):
            def rows(to):
                first = pl.multiple_of(WIDTH * to + columns.start, 128)
                return r.s_qkv.at[:, pl.ds(first, width)]

            dst = r.w_qkv.at[chip_rows, columns]
            stack(lambda to: push(rows(to), dst, S.w_qkv, b, 2 * to + c))
            keep(rows(z), dst, S.w_qkv)

        by_core(send)
        sent_by_core(S.w_qkv, lambda width: r.w_qkv.at[0:144, 0:width])

    def over_plane(dst, at):
        rows = dst.at[group_rows, part]
        peers(lambda k, to: push(rows, rows, at + k, to, s))
        for k in (1, 2, 3):
            sent(at + k, dst.at[0:192, 0:HALF])

    def share(dst, at, onward):
        for k in range(4):
            rows = dst.at[pl.ds(pl.multiple_of(192 * near[k], 16), 192), part]
            if k:
                got(at + k, rows)
            push(rows, rows, onward, b, mate)
        sent(onward, dst.at[:, 0:HALF])

    def line_share(block, at, onward):
        for k in range(4):
            line_got(block, at, k)
            push(block(k), block(k), onward, b, mate)

    got(S.mix_qkv, r.wide_qkv.at[0:24])
    r.s_qkv[...] = r.wide_qkv[...].astype(BF)
    slices_along_line()
    line_gather(token_block, S.tok, rest=False)
    sent(S.tok, r.toks.at[0:3])
    got(S.mix_attn, r.wide_attn.at[0:24])
    r.s_attn[...] = r.wide_attn[...].astype(BF)

    def qkv_over_plane(columns, width):
        got(S.w_qkv, r.w_qkv.at[0:192, 0:width])
        rows = r.w_qkv.at[group_rows, columns]
        peers(lambda k, to: push(rows, rows, S.group_qkv + k, to, s))

    by_core(qkv_over_plane)
    for k in (1, 2, 3):
        sent_by_core(S.group_qkv + k, lambda width: r.w_qkv.at[0:192, 0:width])
    line_gather(token_block, S.tok, near=False)
    for h in range(2):

        @pl.when(c == h)
        def _():
            r.w_attn[chip_rows, 384 * h : 384 * h + 384] = r.s_attn[:, 384 * h : 384 * h + 384]

    line_gather(attn_block, S.w_attn)
    sent(S.w_attn, r.w_attn.at[0:144, 0:HALF])
    line_gather(out_block, S.w_out)
    sent(S.w_out, r.w_out.at[0:3, 0])
    got(S.mix_in, r.wide_in.at[0:24])
    r.s_in[...] = r.wide_in[...].astype(BF)
    peers(
        lambda k, to: push(
            block(r.s_in, WIDTH * to + HALF * c), r.w_in.at[b, z, :, part], S.plane_in, to, s
        )
    )
    keep(block(r.s_in, WIDTH * b + HALF * c), r.w_in.at[b, z, :, part], S.plane_in)
    sent(S.plane_in, r.w_in.at[0:3, 0, :, 0:HALF])

    def hidden_rows(k):
        place = (2 * k + c) * ROWS + lax.broadcasted_iota(jnp.int32, (ROWS, 1), 0)
        return (place >= r.when[1, 0]) & (place < r.when[1, 0] + r.when[2, 0])

    def first_norm(tokens, k):
        x0 = jnp.where(hidden_rows(k), i_vec[8:9, :], tokens.astype(F32))
        normed, inverse = normalize(x0)
        r.n1[k] = normed
        r.inv1[k] = jnp.broadcast_to(inverse, (ROWS, 128))
        return x0

    r.x0[...] = first_norm(i_tok[0], z)

    got(S.mod, r.mod_got)
    r.mod_flat[...] = jnp.zeros((40, 128), F32)
    for k in range(ALL):
        first = 9 * k // 8
        r.mod_flat[first : first + 3, :] += r.mod_got[k, 0:3, :]
    for k in range(6):
        row = jnp.concatenate(
            [r.mod_flat[6 * k + t : 6 * k + t + 1, :] for t in range(6)], axis=1
        )
        r.mod[k : k + 1, :] = row + i_vec[2 + k : 3 + k, :]

    def mod(k):
        return r.mod[k : k + 1, :]

    def vec(k):
        return i_vec[k : k + 1, :]

    r.h1[z] = (r.n1[z] * vec(0) * (1.0 + mod(1)) + mod(0)).astype(BF)
    r.dm[0] = (i_cot[0].astype(F32) * mod(5)).astype(BF)
    peers(lambda k, to: push(r.dm.at[0], r.dm.at[k], S.dm + k, to, s))
    for k in (1, 2, 3):
        sent(S.dm + k, r.dm.at[0])

    lanes = lax.broadcasted_iota(jnp.int32, (ROWS, 128), 1)
    first_half = lanes % HD < HD // 2
    speed = jnp.exp((lanes % (HD // 2)).astype(F32) * (-math.log(10000.0) / (HD // 2)))
    row = lax.broadcasted_iota(jnp.int32, (ROWS, 128), 0)

    def table(k):
        angle = ((2 * k + c) * ROWS + row).astype(F32) * speed
        r.turn[0, k] = jnp.cos(angle)
        sine = jnp.sin(angle)
        r.turn[1, k] = jnp.where(first_half, -sine, sine)

    loop(LINE, table)

    line_relay(token_block, S.tok)

    def qkv_share(columns, width):
        for k in range(4):
            rows = r.w_qkv.at[pl.ds(pl.multiple_of(192 * near[k], 16), 192), columns]
            if k:
                got(S.group_qkv + k, rows)
            push(rows, rows, S.fw_qkv, b, mate)

    by_core(qkv_share)
    sent_by_core(S.fw_qkv, lambda width: r.w_qkv.at[:, 0:width])
    by_core(lambda columns, width: got(S.fw_qkv, r.w_qkv.at[:, 0 : PACK - width]))
    for k in range(5):
        columns = slice(128 * k, 128 * k + 128)
        r.t_w_qkv[columns, :] = r.w_qkv[:, columns].T

    def turned(tile, sign, k):
        other = jnp.where(first_half, pltpu.roll(tile, 96, 1), pltpu.roll(tile, 32, 1))
        return tile * r.turn[0, k] + sign * (other * r.turn[1, k])

    def project(j):
        k = lax.rem(z + j, LINE)

        @pl.when(j > 0)
        def _():
            line_got(token_block, S.tok, k)
            first_norm(r.toks[k], k)
            r.h1[k] = (r.n1[k] * vec(0) * (1.0 + mod(1)) + mod(0)).astype(BF)

        x = dot(r.h1[k], r.w_qkv[:, 0:PACK])
        tiles = [x[:, 128 * t : 128 * t + 128] for t in range(5)]
        tiles[0] = turned(tiles[0], 1.0, k) * 0.125
        tiles[1] = jnp.where(low, turned(tiles[1], 1.0, k) * 0.125, tiles[1])
        tiles[2] = turned(tiles[2], 1.0, k)
        tiles[3] = turned(tiles[3], 1.0, k)
        for t in range(5):
            r.xb[0, k, :, 128 * t : 128 * t + 128] = tiles[t].astype(BF)
        push(r.xb.at[0, k], r.xb.at[1, k], S.xf + k, b, mate)

    loop(4, project)
    line_relay(attn_block, S.w_attn)
    for k in range(4):
        line_got(attn_block, S.w_attn, k)
    over_plane(r.w_attn, S.group_attn)
    for k in range(4):
        sent(S.xf + k, r.xb.at[0, 0])

    for k in range(6):
        columns = slice(128 * k, 128 * k + 128)
        r.t_h1[columns, :] = r.h1[:, :, columns].reshape(512, 128).T
    for k in range(4):
        got(S.xf + k, r.xb.at[0, 0])

    def tile_of(t):
        return r.xb[:, :, :, 128 * t : 128 * t + 128].reshape(1024, 128)

    heads = ((0, 2, 4, True, True), (0, 2, 4, False, False), (1, 3, 1, True, False))

    def queries(head, first, size):
        q_tile, _, _, q_low, _ = heads[head]
        q = r.xb[0, first : first + size, :, 128 * q_tile : 128 * q_tile + 128]
        return jnp.where(low if q_low else ~low, q.reshape(size * 128, 128), jnp.zeros((), BF))

    r.vt[0] = tile_of(4).T
    r.vt[1] = tile_of(1).T
    for half in range(2):
        at = slice(256 * half, 256 * half + 256)
        for head in range(3):
            scores = dot_nt(tile_of(heads[head][1]), queries(head, 2 * half, 2))
            weights = jnp.exp(scores - jnp.max(scores, axis=0, keepdims=True))
            weights = weights * (1.0 / jnp.sum(weights, axis=0, keepdims=True))
            weights = weights.astype(BF)
            r.pt[head, :, at] = weights
            out = dot(r.vt[head // 2], weights)
            if head == 0:
                r.ot[0, 0:64, at] = out[0:64]
            elif head == 1:
                r.ot[0, 64:128, at] = out[64:128]
            else:
                r.ot[1, 0:64, at] = out[64:128]
                r.ot[1, 64:128, at] = jnp.zeros((64, 256), F32)
        for k in (2 * half, 2 * half + 1):
            across = slice(128 * k, 128 * k + 128)
            r.os[k, 0:128, :] = r.ot[0, :, across].T.astype(BF)
            third = r.ot[1, 0:64, across]
            third = jnp.concatenate([third, pltpu.roll(third, 64, 1)], axis=0)
            r.os[k, 128:192, :] = third.T[0:64].astype(BF)
        for to in (2 * half, 2 * half + 1):

            @pl.when(z == to)
            def _():
                keep(r.os.at[to], r.ob.at[z], S.o)

            @pl.when(z != to)
            def _():
                push(r.os.at[to], r.ob.at[z], S.o, b, 2 * to + c)

        if half == 0:
            line_relay(out_block, S.w_out)

    sent(S.o, r.os.at[0:3])
    got(S.plane_in, r.w_in.at[:, 0, :, 0:HALF])
    line_gather(in_block, S.w_in)
    sent(S.w_in, r.w_in.at[0:3, :, :, 0:HALF])
    for k in range(2):
        r.kt[k] = tile_of(2 + k).T
    share(r.w_attn, S.group_attn, S.fw_attn)
    got(S.fw_attn, r.w_attn.at[:, 0:HALF])
    for p in range(4):
        first = 192 * p
        r.t_w_attn[:, 256 * p : 256 * p + 128] = r.w_attn[first : first + 128, :].T
        third = r.w_attn[first + 128 : first + 192, :]
        r.t_w_attn[:, 256 * p + 128 : 256 * p + 256] = jnp.concatenate(
            [third, jnp.zeros_like(third)], axis=0
        ).T
    got(S.o, r.ob)
    a = jnp.zeros((ROWS, WIDTH), F32)
    for p in range(4):
        third = r.ob[p, 128:192, :].astype(F32)
        third = jnp.concatenate([third, pltpu.roll(third, 64, 1)], axis=0)
        r.o2[p] = jnp.where(low, third, 0.0).astype(BF)
        a += dot(r.ob[p, 0:128, :], r.w_attn[192 * p : 192 * p + 128, :])
        a += dot(r.o2[p, :, 0:64], r.w_attn[192 * p + 128 : 192 * p + 192, :])
    r.a[...] = a
    x1 = r.x0[...] + mod(2) * a
    r.x1[...] = x1
    n2, inv2 = normalize(x1)
    r.n2[...] = n2
    r.inv2[...] = jnp.broadcast_to(inv2, (ROWS, 128))
    r.h2[0] = (n2 * vec(1) * (1.0 + mod(4)) + mod(3)).astype(BF)
    peers(lambda k, to: push(r.h2.at[0], r.h2.at[k], S.h2 + k, to, s))
    for k in (1, 2, 3):
        sent(S.h2 + k, r.h2.at[0])
    line_relay(in_block, S.w_in)
    line_share(out_block, S.w_out, S.fw_out)
    sent(S.fw_out, r.w_out.at[:, 0])
    got(S.fw_out, r.w_out.at[:, 0])

    def feed_back(k):
        @pl.when(k > 0)
        def _():
            got(S.dm + k, r.dm.at[0])

        r.back[k] = dot_nt(r.dm[k], r.w_out[...].reshape(WIDTH, WIDTH))

    loop(4, feed_back)
    line_share(in_block, S.w_in, S.fw_in)
    sent(S.fw_in, r.w_in.at[:, :, :, 0:HALF])
    got(S.fw_in, r.w_in.at[:, :, :, 0:HALF])

    def feed(k):
        u = dot(r.h2[k], r.w_in[...].reshape(WIDTH, WIDTH))
        slope = 0.7978845608028654
        cube = 0.044715
        t = jnp.tanh(slope * (u + cube * u * u * u))
        r.gb[k] = (0.5 * u * (1.0 + t)).astype(BF)
        bend = 0.5 * (1.0 + t) + 0.5 * u * (1.0 - t * t) * (slope * (1.0 + 3.0 * cube * u * u))
        r.du[k] = (r.back[k] * bend).astype(BF)
        r.dhs[k] = dot_nt(r.du[k], r.w_in[...].reshape(WIDTH, WIDTH)).astype(BF)

    feed(0)
    for k in (1, 2, 3):
        slot, to = toward(k)
        got(S.h2 + slot, r.h2.at[0])
        feed(slot)
        push(r.dhs.at[slot], r.dhr.at[slot], S.dh2, to, s)
    sent(S.dh2, r.dhs.at[0:3])
    def gather(own, others):
        total = own[0].astype(F32)
        for k in (1, 2, 3):
            total += others[k].astype(F32)
        return total

    for k in range(2):
        rows = slice(384 * k, 384 * k + 384)
        result = dot_tn(r.gb[:, :, rows].reshape(512, 384), r.dm[...].reshape(512, 768))
        r.g_out[2 * k : 2 * k + 2] = result.astype(BF).reshape(2, 2, 96, 768)
    push(r.g_out.at[:, 1 - c], r.p_out, S.pair_out, b, mate)
    sent(S.pair_out, r.p_out)

    def to_mate(grad, dst, at):
        push(grad.at[1 - c], dst, at, b, mate)
        sent(at, dst)

    def pair_sum(grad, pair, at):
        got(at, pair)
        grad[c] = (grad[c].astype(F32) + pair[...].astype(F32)).astype(BF)

    def plane_sum(grad, dst, at, packed=False):
        def send(columns, width):
            def rows(to):
                return grad.at[c, pl.ds(pl.multiple_of(192 * to, 16), 192), 0:width]

            peers(lambda k, to: push(rows(to), dst.at[k, :, 0:width], at, to, s))
            keep(rows(b), dst.at[0, :, 0:width], at)

        if packed:
            by_core(send)
            sent_by_core(at, lambda width: dst.at[0:3, :, 0:width])
        else:
            send(None, HALF)
            sent(at, dst.at[0:3])

    def line_sum(src, total, dst, first, at, packed=False):
        def send(columns, width):
            got(first, src.at[:, :, 0:width])
            total[...] = (
                (src[0].astype(F32) + src[1].astype(F32))
                + (src[2].astype(F32) + src[3].astype(F32))
            ).astype(BF)

            def rows(to):
                return total.at[pl.ds(pl.multiple_of(48 * to, 16), 48), 0:width]

            stack(lambda to: push(rows(to), dst.at[z, :, 0:width], at, b, 2 * to + c))
            keep(rows(z), dst.at[z, :, 0:width], at)

        if packed:
            by_core(send)
            sent_by_core(at, lambda width: dst.at[0:3, :, 0:width])
        else:
            send(None, HALF)
            sent(at, dst.at[0:3])

    def trade(total, final, at):
        push(total.at[:, mate24], final.at[:, c], at, b, mate)
        sent(at, final.at[:, 0])
        final[:, c] = total[:, own24, :]

    def in_product(k):
        rows = slice(384 * k, 384 * k + 384)
        result = dot_tn(r.h2[:, :, rows].reshape(512, 384), r.du[...].reshape(512, 768)).astype(BF)
        for h in range(2):
            r.g_in[h, 2 * k : 2 * k + 2] = result[:, 384 * h : 384 * h + 384].reshape(2, 4, 48, 384)

    in_product(0)

    got(S.pair_out, r.p_out)
    for k in range(4):
        r.g_out[k, c] = (r.g_out[k, c].astype(F32) + r.p_out[k].astype(F32)).astype(BF)

    def out_rows(k):
        return r.g_out.at[k, c]

    for j in (0, 1):
        line_add(j, out_rows, r.r_out, r.via_out, S.line_out)
    in_product(1)
    to_mate(r.g_in, r.p_in, S.pair_in)

    def add_out():
        k = line_order(2)
        r.g_out[k, c] = (r.g_out[k, c].astype(F32) + r.via_out[...].astype(F32)).astype(BF)

    got(S.dh2, r.dhr.at[0:3])
    dh = gather(r.dhs, r.dhr)
    n2 = r.n2[...]
    inv2 = r.inv2[:, 0:1]
    r.early[...] = jnp.zeros((8, 768), F32)
    r.early[2:3, :] = jnp.sum(dh, axis=0, keepdims=True)
    both = jnp.sum(dh * n2, axis=0, keepdims=True)
    r.early[3:4, :] = both * vec(1)
    r.early[0:1, :] = both * (1.0 + mod(4))
    grad = dh * ((1.0 + mod(4)) * vec(1))
    dx1 = i_cot[0].astype(F32) + norm_back(n2, inv2, grad)
    r.dx1[...] = dx1
    r.early[1:2, :] = jnp.sum(dx1 * r.a[...], axis=0, keepdims=True)
    r.das[...] = (dx1 * mod(2)).astype(BF)
    def make_do(to):
        columns = pl.ds(pl.multiple_of(256 * to, 256), 256)
        result = dot(r.das[...], r.t_w_attn[:, columns])
        r.dos[to, 0:128, :] = result[:, 0:128].astype(BF)
        third = result[:, 128:256]
        third = jnp.where(low, third[0:64], pltpu.roll(third[64:128], 64, 1))
        r.dos[to, 128:192, :] = third.astype(BF)

    def send_do(to):
        make_do(to)
        push(r.dos.at[to], r.dob.at[z], S.do, b, 2 * to + c)

    stack(send_do)
    make_do(z)
    keep(r.dos.at[z], r.dob.at[z], S.do)
    sent(S.do, r.dos.at[0:3])
    for t in range(3):
        at = slice(256 * t, 256 * t + 256)
        mm = dot(r.gb[...].reshape(512, WIDTH), r.w_out[:, :, :, at].reshape(WIDTH, 256))
        r.mms[:, :, at] = mm.astype(BF).reshape(4, ROWS, 256)
    peers(lambda k, to: push(r.mms.at[k], r.mmr.at[k], S.mm, to, s))
    sent(S.mm, r.mms.at[0:3])

    for p in range(4):
        for rows, left_side in (
            (slice(192 * p, 192 * p + 128), r.ob[p, 0:128, :]),
            (slice(192 * p + 128, 192 * p + 192), r.o2[p]),
        ):
            result = dot_tn(left_side, r.das[...])[0 : rows.stop - rows.start].astype(BF)
            r.g_attn[0, rows, :] = result[:, 0:HALF]
            r.g_attn[1, rows, :] = result[:, HALF:WIDTH]
    to_mate(r.g_attn, r.p_attn, S.pair_attn)

    def small_sum(src, pair, line, plane, whole, at):
        def first():
            push(src, pair, at, b, mate)
            sent(at, src)

        def second():
            got(at, pair)
            total = src[...] + pair[...]
            line[z] = (1 - c) * total[:, 0:HALF] + c * total[:, HALF:WIDTH]
            stack(lambda to: push(line.at[z], line.at[z], at + 1, b, 2 * to + c))
            sent(at + 1, line.at[0:3])

        def third():
            got(at + 1, line.at[0:3])
            plane[b] = (line[0] + line[1]) + (line[2] + line[3])
            peers(lambda k, to: push(plane.at[b], plane.at[b], at + 2, to, s))
            sent(at + 2, plane.at[0:3])

        def fourth():
            got(at + 2, plane.at[0:3])
            whole[c] = plane[...]
            push(plane, whole.at[c], at + 3, b, mate)
            sent(at + 3, plane)

        def rows(k):
            return jnp.concatenate([whole[0, k], whole[1, k]], axis=1)

        return first, second, third, fourth, rows

    early_steps = small_sum(
        r.early, r.early_pair, r.early_line, r.early_plane, r.early_all, S.early
    )
    late_steps = small_sum(r.late, r.late_pair, r.late_line, r.late_plane, r.late_all, S.late)

    pair_sum(r.g_in, r.p_in, S.pair_in)
    line_via(r.via_out, S.line_out, add_out)
    for j in (2, 3):
        line_add(j, out_rows, r.r_out, r.via_out, S.line_out)
    sent(S.line_out, r.r_out.at[0:3])

    def in_rows(k):
        return r.g_in.at[c, :, k]

    for j in (0, 1):
        line_add(j, in_rows, r.r_in, r.via_in, S.line_in)

    def add_in():
        k = line_order(2)
        r.g_in[c, :, k] = (r.g_in[c, :, k].astype(F32) + r.via_in[...].astype(F32)).astype(BF)

    pair_sum(r.g_attn, r.p_attn, S.pair_attn)
    plane_sum(r.g_attn, r.q_attn, S.plane_attn)

    got(S.do, r.dob)
    dot0 = r.dob[:, 0:128, :].reshape(512, 128)
    third = r.dob[:, 128:192, :].astype(F32).reshape(256, 128)
    other_rows = jnp.where(low, pltpu.roll(third, 64, 1), 0.0).reshape(4, 64, 128)
    third = jnp.where(low, third, 0.0).reshape(4, 64, 128)
    dot1 = jnp.concatenate([third, other_rows], axis=1).reshape(512, 128)
    zero = jnp.zeros((), BF)
    moved = pltpu.roll(dot1, 64, 1).astype(BF)
    grads = (jnp.where(low, dot0, zero), jnp.where(low, zero, dot0), moved)
    product = dot0.astype(F32).T * r.ot[0]
    deltas = (
        jnp.sum(product[0:64], axis=0, keepdims=True),
        jnp.sum(product[64:128], axis=0, keepdims=True),
        jnp.sum(dot1.T * r.ot[1], axis=0, keepdims=True),
    )
    for head in range(3):
        values = tile_of(heads[head][2])
        for half in range(2):
            at = slice(256 * half, 256 * half + 256)
            dp = dot_nt(values, grads[head][at])
            r.dst[head, :, at] = (
                r.pt[head, :, at].astype(F32) * (dp - deltas[head][:, at])
            ).astype(BF)

    def key_grads(rows):
        dk = [dot(r.dst[head, rows, :], queries(head, 0, 4)) for head in range(3)]
        dv = [dot(r.pt[head, rows, :], grads[head]) for head in range(3)]
        return (dv[2], dk[0] + dk[1], dk[2], dv[0] + dv[1])

    line_via(r.via_in, S.line_in, add_in)
    for j in (2, 3):
        line_add(j, in_rows, r.r_in, r.via_in, S.line_in)
    sent(S.line_in, r.r_in.at[0:3])
    for t, tile in enumerate(key_grads(slice(512, 1024))):
        r.gps[:, 128 * t : 128 * t + 128] = tile.astype(BF)
    push(r.gps, r.gpr, S.gp, b, mate)
    sent(S.gp, r.gps)
    for t, tile in enumerate(key_grads(slice(0, 512))):
        r.ga[:, 128 * t + 128 : 128 * t + 256] = tile
    for half in range(2):
        at = slice(256 * half, 256 * half + 256)
        turned_q = [dot(r.kt[head // 2], r.dst[head, :, at]) for head in range(3)]
        top = jnp.concatenate([turned_q[0][0:64], turned_q[1][64:128]], axis=0)
        r.ga[at, 0:128] = top.T * 0.125
        r.ga[at, 128:256] += turned_q[2].T * 0.125
    got(S.gp, r.gpr)

    def dh1_rows(k):
        return r.d1s.at[k]

    def back_turn(k):
        rows = pl.ds(pl.multiple_of(128 * k, 128), 128)
        tiles = [r.ga[rows, 0:128]] + [
            r.ga[rows, 128 * t : 128 * t + 128]
            + r.gpr[rows, 128 * t - 128 : 128 * t].astype(F32)
            for t in range(1, 5)
        ]
        tiles[0] = turned(tiles[0], -1.0, k)
        tiles[1] = jnp.where(low, turned(tiles[1], -1.0, k), tiles[1])
        tiles[2] = turned(tiles[2], -1.0, k)
        tiles[3] = turned(tiles[3], -1.0, k)
        for t in range(5):
            r.dqkv[k, :, 128 * t : 128 * t + 128] = tiles[t].astype(BF)
        r.dqkv[k, :, PACK:WIDTH] = jnp.zeros((128, 128), BF)

    back_turn(line_order(0))

    def unproject(j):
        k = line_order(j)
        partial_sum = dot(r.dqkv[k, :, 0:PACK], r.t_w_qkv[...])
        r.d1s[k] = partial_sum.astype(BF)
        if j == 2:

            def add():
                r.d1s[k] = (partial_sum + r.via_dh1[...].astype(F32)).astype(BF)

            line_via(r.via_dh1, S.dh1, add)
        line_add(j, dh1_rows, r.d1r, r.via_dh1, S.dh1)
        n = r.n1[k]
        e = partial_sum * ((1.0 + mod(1)) * vec(0))
        weight = jnp.where(hidden_rows(k), r.inv1[k][:, 0:1], 0.0)
        centred = (
            e
            - jnp.mean(e, axis=-1, keepdims=True)
            - n * jnp.mean(e * n, axis=-1, keepdims=True)
        )
        r.late[0:1, :] += jnp.sum(partial_sum * n, axis=0, keepdims=True)
        r.late[1:2, :] += jnp.sum(partial_sum, axis=0, keepdims=True)
        r.late[3:4, :] += jnp.sum(weight * centred, axis=0, keepdims=True)

    r.late[...] = jnp.zeros((4, 768), F32)
    r.late[3:4, :] = jnp.sum(
        jnp.where(hidden_rows(z), r.dx1[...], 0.0), axis=0, keepdims=True
    )
    unproject(0)
    for j in (1, 2, 3):
        back_turn(line_order(j))

    def qkv_rows(k):
        rows = pl.ds(pl.multiple_of(128 * k, 128), 128)
        result = dot(r.t_h1[rows, :], r.dqkv[...].reshape(512, WIDTH)).astype(BF)
        r.g_qkv[0, rows, :] = result[:, 0:HALF]
        r.g_qkv[1, rows, :] = result[:, HALF:WIDTH]

    loop(6, qkv_rows)
    to_mate(r.g_qkv, r.p_qkv, S.pair_qkv)
    unproject(1)
    pair_sum(r.g_qkv, r.p_qkv, S.pair_qkv)
    plane_sum(r.g_qkv, r.q_qkv, S.plane_qkv, True)
    got(S.mm, r.mmr.at[0:3])
    mm = gather(r.mms, r.mmr)
    o_y[...] = (r.x1[...] + mod(5) * mm).astype(BF)
    r.early[4:5, :] = jnp.sum(i_cot[0].astype(F32) * mm, axis=0, keepdims=True)
    early_steps[0]()
    unproject(2)
    unproject(3)
    sent(S.dh1, r.d1s.at[0:3])
    both = r.late[0:1, :]
    r.late[2:3, :] = both * vec(0)
    r.late[0:1, :] = both * (1.0 + mod(1))
    late_steps[0]()
    early_steps[1]()
    line_sum(r.q_attn, r.m_attn, r.r_attn, S.plane_attn, S.line_attn)
    late_steps[1]()

    line_done(r.r_in, S.line_in)
    r.m_in[...] = (
        (r.r_in[0].astype(F32) + r.r_in[1].astype(F32))
        + (r.r_in[2].astype(F32) + r.r_in[3].astype(F32))
    ).astype(BF)
    peers(lambda k, to: push(r.m_in.at[to], r.u_in.at[b], S.slice_in, to, s))
    keep(r.m_in.at[b], r.u_in.at[b], S.slice_in)
    sent(S.slice_in, r.u_in.at[0:3])
    line_sum(r.q_qkv, r.m_qkv, r.r_qkv, S.plane_qkv, S.line_qkv, True)
    early_steps[2]()
    late_steps[2]()

    line_done(r.d1r, S.dh1)
    dh = (r.d1r[0].astype(F32) + r.d1r[1].astype(F32)) + (
        r.d1r[2].astype(F32) + r.d1r[3].astype(F32)
    )
    n1 = r.n1[z]
    grad = dh * ((1.0 + mod(1)) * vec(0))
    dx0 = r.dx1[...] + norm_back(n1, r.inv1[z][:, 0:1], grad)
    o_dx[...] = jnp.where(hidden_rows(z), 0.0, dx0)
    early_steps[3]()
    late_steps[3]()

    line_done(r.r_out, S.line_out)
    total = (r.r_out[0].astype(F32) + r.r_out[1].astype(F32)) + (
        r.r_out[2].astype(F32) + r.r_out[3].astype(F32)
    )
    o_gout[...] = total
    squares = total * total
    squares = jnp.sum(squares[:, 0:128] + squares[:, 128:256] + squares[:, 256:384]
                      + squares[:, 384:512] + squares[:, 512:640] + squares[:, 640:768],
                      axis=0, keepdims=True)

    def fold(value):
        total = value[:, 0:128] * value[:, 0:128]
        for t in range(1, value.shape[1] // 128):
            total += value[:, 128 * t : 128 * t + 128] * value[:, 128 * t : 128 * t + 128]
        return jnp.sum(total, axis=0, keepdims=True)

    got(S.slice_in, r.u_in)
    r.t_in[...] = r.u_in[...].astype(F32)
    for p in range(4):
        squares += fold(r.t_in[p])
    trade(r.t_in, r.f_in, S.last_in)
    got(S.line_attn, r.r_attn)
    r.t_attn[0] = (r.r_attn[0].astype(F32) + r.r_attn[1].astype(F32)) + (
        r.r_attn[2].astype(F32) + r.r_attn[3].astype(F32)
    )
    squares += fold(r.t_attn[0])
    trade(r.t_attn, r.f_attn, S.last_attn)
    by_core(lambda columns, width: got(S.line_qkv, r.r_qkv.at[:, :, 0:width]))
    r.t_qkv[...] = r.r_qkv[...].astype(F32)
    trade(r.t_qkv, r.f_qkv, S.last_qkv)
    for p in range(4):
        squares += fold(r.t_qkv[p])
    r.sq[me] = squares

    def send_sq(k):
        other = lax.rem(me + k, ALL)
        push(r.sq.at[me], r.sq.at[me], S.sq, lax.div(other, SEQ), lax.rem(other, SEQ))

    loop(ALL, send_sq, 1)
    sent(S.sq, r.sq.at[0:31])
    got(S.last_in, r.f_in.at[:, 0])
    got(S.last_attn, r.f_attn.at[:, 0])
    for h in range(2):
        for p in range(4):
            value = r.f_in[p, h]
            o_gin[:, 768 * p + 384 * h : 768 * p + 384 * h + 384] = value
        value = r.f_attn[0, h]
        o_gattn[:, 384 * h : 384 * h + 384] = value
    got(S.last_qkv, r.f_qkv.at[:, 0])
    where = {which: index for index, which in enumerate(HALVES) if which is not None}

    def packed_half(chunk, high):
        kind, rest = chunk // 12, chunk % 12
        index = where[(kind, rest % 3)]
        t = index // 2
        tile = r.f_qkv[rest // 3, t // 3, :, t % 3 * 128 : t % 3 * 128 + 128]
        return tile if index % 2 == high else pltpu.roll(tile, 64, 1)

    for t in range(18):
        o_gqkv[:, 128 * t : 128 * t + 128] = jnp.where(
            low, packed_half(2 * t, 0), packed_half(2 * t + 1, 1)
        )
    got(S.early + 3, r.early_all.at[0])
    got(S.late + 3, r.late_all.at[0])
    early_rows = [early_steps[4](k) for k in range(4)]
    late_rows = [late_steps[4](k) for k in range(4)]
    mods = []
    for k in range(4):
        early, late = early_rows[k], late_rows[k]
        rows = jnp.concatenate([late[1:3], early[1:5], jnp.zeros((2, 768), F32)], axis=0)
        for n in range(6):
            for m in range(6):
                r.dmod_flat[k, 6 * n + m : 6 * n + m + 1, :] = rows[
                    n : n + 1, 128 * m : 128 * m + 128
                ]
        mods.append(rows)
    gain = jnp.concatenate(
        [
            sum(late_rows[k][0:1] for k in range(4)),
            sum(early_rows[k][0:1] for k in range(4)),
            (mods[0] + mods[1] + mods[2] + mods[3])[0:6],
        ],
        axis=0,
    )
    mask_row = sum(late_rows[k][3:4] for k in range(4))
    gains = jnp.concatenate([gain, mask_row, jnp.zeros((7, 768), F32)], axis=0)
    masters = jnp.concatenate([i_vec[...], jnp.zeros((7, 768), F32)], axis=0)
    own = lax.rem(WIDTH - 24 * me, WIDTH)
    o_gvec[...] = pltpu.roll(gains, own, 1)[:, 0:128]
    o_vec[...] = pltpu.roll(masters, own, 1)[:, 0:128]
    r.mod_pad[...] = jnp.zeros((8, 384), F32)
    window = lax.div(wide * me, 128)
    for k in range(4):
        rows = r.dmod_flat[k, pl.ds(window, 3), :]
        for m in range(3):
            r.mod_pad[k : k + 1, 128 * m : 128 * m + 128] = rows[m : m + 1, :]
    o_dmod[...] = pltpu.roll(r.mod_pad[...], lax.rem(384 - lax.rem(wide * me, 128), 384), 1)[:, 0:256]
    small = jnp.sum(gain * gain) + jnp.sum(mask_row * mask_row)
    conds = [r.conds_all[k][0:1].astype(BF).astype(F32) for k in range(4)]
    for k in range(4):
        for m in range(k, 4):
            term = jnp.sum(mods[k] * mods[m]) * jnp.sum(conds[k] * conds[m])
            small += term if m == k else 2.0 * term
    got(S.sq, r.sq.at[0:31])
    total = r.sq[0]
    for k in range(1, ALL):
        total += r.sq[k]
    o_norm[...] = jnp.broadcast_to(jnp.sqrt(jnp.sum(total) + small), (8, 128))

    for drained in drains:
        drained()


def run_layer(*args):
    shapes = (
        ((ROWS, WIDTH), BF),
        ((ROWS, WIDTH), F32),
        ((8, 128), F32),
        ((24, 3 * WIDTH), F32),
        ((24, WIDTH), F32),
        ((24, 4 * WIDTH), F32),
        ((96, WIDTH), F32),
        ((8, 256), F32),
        ((16, 128), F32),
        ((16, 128), F32),
        ((8, 128), F32),
    )
    whole = pl.BlockSpec(memory_space=pltpu.VMEM)
    return pl.pallas_call(
        layer_kernel,
        out_shape=[jax.ShapeDtypeStruct(shape, kind) for shape, kind in shapes],
        in_specs=[pl.BlockSpec(memory_space=pl.ANY)] * len(args),
        out_specs=[whole] * len(shapes),
        scratch_shapes=[pltpu.VMEM(shape, kind) for shape, kind in SCRATCH.values()]
        + [pltpu.SMEM((3, 1), jnp.int32)]
        + [pltpu.SemaphoreType.DMA((SEM_COUNT,)), pltpu.SemaphoreType.DMA((SEM_COUNT,))],
        compiler_params=pltpu.CompilerParams(
            collective_id=0, has_side_effects=True, vmem_limit_bytes=60 * 1024 * 1024
        ),
    )(*args)


HELD = (2, 8, 9, 7, 10, 3, 4, 5, 6)


def finish_kernel(*refs):
    sources, outs, refs = refs[:28], refs[28:49], refs[49:]
    near, results, load_sems, store_sems = refs[:28], refs[28:46], refs[46], refs[47]
    norm, g_vec, own_vec, dmod, conds = near[:5]
    weights, moments = (own_vec, *near[9:14]), near[14:26]

    order = list(range(5)) + [14, 15, 9, 16, 17]
    for k in range(2, 6):
        order += [3 + k, 8 + k, 14 + 2 * k, 15 + 2 * k]
    loads = {}
    for n in order:
        source = sources[HELD[n]] if n < 9 else sources[n + 2]
        loads[n] = pltpu.make_async_copy(source, near[n], load_sems.at[n])
        loads[n].start()
    for n in (26, 27):
        loads[n] = pltpu.make_async_copy(sources[n - 26], near[n], load_sems.at[n])
        loads[n].start()
    for n in order[:10]:
        loads[n].wait()
    outs[2][0, 0] = norm[0, 0]
    clip = jnp.minimum(1.0, CLIP / (norm[0:1, 0:1] + 1e-06))
    wide, narrow = near[9].shape[0], moments[0].shape[1]
    rounded = conds[...].astype(BF).astype(F32)
    turned_mod = dmod[...].T
    g_ada = turned_mod[0:wide, 0:1] * rounded[0:1, :]
    for k in range(1, 4):
        g_ada += turned_mod[0:wide, k : k + 1] * rounded[k : k + 1, :]
    stores = []
    for k in range(6):
        if k > 1:
            for n in order[2 + 4 * k : 6 + 4 * k]:
                loads[n].wait()
        grad = g_vec[0:9, 0:narrow] if k == 0 else g_ada if k == 1 else near[3 + k][...]
        updated = adam_step(
            weights[k][...] if k else own_vec[0:9, 0:narrow],
            grad * clip,
            moments[2 * k][...],
            moments[2 * k + 1][...],
            RATE if k else RATE_VECTORS,
            DECAY if k else 0.0,
        )
        for n in range(3):
            at = 3 * k + n
            results[at][...] = updated[n]
            stores.append(pltpu.make_async_copy(results[at], outs[3 + at], store_sems.at[at]))
            stores[-1].start()
    for n in (26, 27):
        loads[n].wait()
        stores.append(pltpu.make_async_copy(near[n], outs[n - 26].at[0], store_sems.at[n - 8]))
        stores[-1].start()
    for copy in stores:
        copy.wait()


def run_finish(partial_results, weights, moments):
    shapes = [((1, ROWS, WIDTH), BF), ((1, ROWS, WIDTH), F32), ((1, 1), F32)]
    for moment in moments[::2]:
        shapes += [(moment.shape, F32)] * 3
    far = pl.BlockSpec(memory_space=pl.ANY)
    specs = [far] * len(shapes)
    specs[2] = pl.BlockSpec(memory_space=pltpu.SMEM)
    near = [partial_results[k] for k in HELD] + [*weights, *moments, *partial_results[:2]]
    args = (*partial_results, *weights, *moments)
    return pl.pallas_call(
        finish_kernel,
        out_shape=[jax.ShapeDtypeStruct(shape, kind) for shape, kind in shapes],
        in_specs=[far] * len(args),
        out_specs=specs,
        scratch_shapes=[pltpu.VMEM(array.shape, array.dtype) for array in near]
        + [pltpu.VMEM(shape, kind) for shape, kind in shapes[3:]]
        + [pltpu.SemaphoreType.DMA((28,)), pltpu.SemaphoreType.DMA((20,))],
        compiler_params=pltpu.CompilerParams(vmem_limit_bytes=60 * 1024 * 1024),
    )(*args)


def slices(
    tokens_in,
    cotangent,
    timesteps,
    span_start,
    span_len,
    vectors,
    w_ada,
    w_qkv,
    w_attn,
    w_in,
    w_out,
    m_vec,
    v_vec,
    m_ada,
    v_ada,
    m_qkv,
    v_qkv,
    m_attn,
    v_attn,
    m_in,
    v_in,
    m_out,
    v_out,
):
    partial_results = run_layer(
        timesteps,
        span_start,
        span_len,
        tokens_in,
        cotangent,
        vectors,
        w_ada.T,
        w_qkv,
        w_attn,
        w_in,
        w_out,
    )
    moments = (
        m_vec,
        v_vec,
        m_ada.T,
        v_ada.T,
        m_qkv,
        v_qkv,
        m_attn,
        v_attn,
        m_in,
        v_in,
        m_out,
        v_out,
    )
    results = run_finish(partial_results, (w_ada.T, w_qkv, w_attn, w_in, w_out), moments)
    ada_results = [result.T for result in results[6:9]]
    return (*results[:2], results[2].reshape(()), *results[3:6], *ada_results, *results[9:])


def solution(mesh):
    in_specs = (
        P("dp", "seq", None),
        P("dp", "seq", None),
        P("dp"),
        P("dp"),
        P("dp"),
        P(),
        P(None, ("dp", "seq")),
        P(("dp", "seq"), None),
        P(("dp", "seq"), None),
        P(("dp", "seq"), None),
        P(("dp", "seq"), None),
        P(None, ("dp", "seq")),
        P(None, ("dp", "seq")),
        P(None, ("dp", "seq")),
        P(None, ("dp", "seq")),
        P(("dp", "seq"), None),
        P(("dp", "seq"), None),
        P(("dp", "seq"), None),
        P(("dp", "seq"), None),
        P(("dp", "seq"), None),
        P(("dp", "seq"), None),
        P(("dp", "seq"), None),
        P(("dp", "seq"), None),
    )
    out_specs = (
        P("dp", "seq", None),
        P("dp", "seq", None),
        P(),
        P(None, ("dp", "seq")),
        P(None, ("dp", "seq")),
        P(None, ("dp", "seq")),
        P(None, ("dp", "seq")),
        P(None, ("dp", "seq")),
        P(None, ("dp", "seq")),
        P(("dp", "seq"), None),
        P(("dp", "seq"), None),
        P(("dp", "seq"), None),
        P(("dp", "seq"), None),
        P(("dp", "seq"), None),
        P(("dp", "seq"), None),
        P(("dp", "seq"), None),
        P(("dp", "seq"), None),
        P(("dp", "seq"), None),
        P(("dp", "seq"), None),
        P(("dp", "seq"), None),
        P(("dp", "seq"), None),
    )
    sizes = dict(mesh.shape)
    local = slices if (sizes["dp"], sizes["seq"]) == (4, 8) else plain
    return jax.shard_map(local, mesh=mesh, in_specs=in_specs, out_specs=out_specs, check_vma=False)
```

```python
from functools import partial
import math
from types import SimpleNamespace

import jax
import jax.numpy as jnp
from jax import lax
from jax.experimental import pallas as pl
from jax.experimental.pallas import tpu as pltpu
from jax.sharding import PartitionSpec as P

HD = 64
COND = 128
STEP = 10


BETA_ONE = 0.9
BETA_TWO = 0.999
ADAM_EPS = 1e-08
RATE = 0.1
RATE_VECTORS = 0.3
DECAY = 0.01
CLIP = 1.0
NORM_EPS = 1e-05


def cond_input(timesteps):
    half_cond = COND // 2
    freqs = jnp.exp(jnp.arange(half_cond, dtype=jnp.float32) * (-math.log(10000.0) / half_cond))
    angles = timesteps.astype(jnp.float32)[:, None] * freqs[None, :]
    return jax.nn.silu(jnp.concatenate([jnp.cos(angles), jnp.sin(angles)], axis=1))


def rotary_tables(positions):
    half_head = HD // 2
    inverse = jnp.exp(jnp.arange(half_head, dtype=jnp.float32) * (-math.log(10000.0) / half_head))
    angles = positions.astype(jnp.float32)[:, None] * inverse[None, :]
    return (jnp.cos(angles), jnp.sin(angles))


def rotate(values, cosines, sines):
    half_head = values.shape[-1] // 2
    first = values[..., :half_head]
    second = values[..., half_head:]
    cos_b = cosines[:, None, :]
    sin_b = sines[:, None, :]
    return jnp.concatenate(
        [first * cos_b - second * sin_b, second * cos_b + first * sin_b], axis=-1
    )


def rotate_back(grads, cosines, sines):
    half_head = grads.shape[-1] // 2
    first = grads[..., :half_head]
    second = grads[..., half_head:]
    cos_b = cosines[:, None, :]
    sin_b = sines[:, None, :]
    return jnp.concatenate(
        [first * cos_b + second * sin_b, second * cos_b - first * sin_b], axis=-1
    )


def normalize(values):
    centre = jnp.mean(values, axis=-1, keepdims=True)
    centred = values - centre
    inverse = lax.rsqrt(jnp.mean(centred * centred, axis=-1, keepdims=True) + NORM_EPS)
    return (centred * inverse, inverse)


def norm_back(normed, inverse, grad):
    return inverse * (
        grad
        - jnp.mean(grad, axis=-1, keepdims=True)
        - normed * jnp.mean(grad * normed, axis=-1, keepdims=True)
    )


def split_kv(block, width):
    seqs, block_rows = (block.shape[0], block.shape[1])
    keys = block[..., :width].reshape(seqs, block_rows, width // HD, HD)
    values = block[..., width:].reshape(seqs, block_rows, width // HD, HD)
    return (keys, values)


def attend_piece(carry, piece, queries, width, factor):
    piece_rows = piece.shape[1]
    size = math.gcd(piece_rows, 512)

    def attend_one_block(index, state):
        running, denom, accum = state
        block = lax.dynamic_slice_in_dim(piece, index * size, size, 1)
        keys, values = split_kv(block, width)
        scores = (
            jnp.einsum("sqhd,skhd->shqk", queries, keys, preferred_element_type=jnp.float32)
            * factor
        )
        highest = jnp.maximum(running, jnp.max(scores, axis=-1))
        shrink = jnp.exp(running - highest)
        weights = jnp.exp(scores - highest[..., None])
        denom = denom * shrink + jnp.sum(weights, axis=-1)
        accum = accum * shrink[..., None] + jnp.einsum(
            "shqk,skhd->shqd",
            weights.astype(jnp.bfloat16),
            values,
            preferred_element_type=jnp.float32,
        )
        return (highest, denom, accum)

    return lax.fori_loop(0, piece_rows // size, attend_one_block, carry)


def block_grads(block, queries, grad_out, logsum, delta, width, factor):
    keys, values = split_kv(block, width)
    scores = (
        jnp.einsum("sqhd,skhd->shqk", queries, keys, preferred_element_type=jnp.float32) * factor
    )
    probs = jnp.exp(scores - logsum[..., None])
    dprobs = jnp.einsum("sqhd,skhd->shqk", grad_out, values, preferred_element_type=jnp.float32)
    dscores = (probs * (dprobs - delta[..., None])).astype(jnp.bfloat16)
    return (keys, probs, dscores)


def query_grads(kv_all, queries, grad_out, logsum, delta, width, factor):
    total_rows = kv_all.shape[1]
    size = math.gcd(total_rows, 512)

    def query_one_block(index, accum):
        block = lax.dynamic_slice_in_dim(kv_all, index * size, size, 1)
        keys, probs, dscores = block_grads(block, queries, grad_out, logsum, delta, width, factor)
        return accum + factor * jnp.einsum(
            "shqk,skhd->sqhd", dscores, keys, preferred_element_type=jnp.float32
        )

    return lax.fori_loop(
        0, total_rows // size, query_one_block, jnp.zeros(queries.shape, jnp.float32)
    )


def key_grads(kv_all, queries, grad_out, logsum, delta, width, factor, count):
    size = math.gcd(count, 512)
    seqs = queries.shape[0]

    def key_one_block(index, accum):
        block = lax.dynamic_slice_in_dim(kv_all, index * size, size, 1)
        keys, probs, dscores = block_grads(block, queries, grad_out, logsum, delta, width, factor)
        grad_vals = jnp.einsum(
            "shqk,sqhd->skhd",
            probs.astype(jnp.bfloat16),
            grad_out,
            preferred_element_type=jnp.float32,
        )
        grad_keys = factor * jnp.einsum(
            "shqk,sqhd->skhd", dscores, queries, preferred_element_type=jnp.float32
        )
        joined = jnp.concatenate(
            [grad_keys.reshape(seqs, size, width), grad_vals.reshape(seqs, size, width)], axis=-1
        )
        return lax.dynamic_update_slice_in_dim(
            accum, jnp.transpose(joined, (1, 0, 2)), index * size, 0
        )

    initial = jnp.zeros((count, seqs, 2 * width), jnp.float32)
    return lax.fori_loop(0, count // size, key_one_block, initial)


def adam_step(weight, grad, first, second, rate, decay_rate):
    new_first = BETA_ONE * first + (1.0 - BETA_ONE) * grad
    new_second = BETA_TWO * second + (1.0 - BETA_TWO) * grad * grad
    fixed_first = new_first / (1.0 - BETA_ONE**STEP)
    fixed_second = new_second / (1.0 - BETA_TWO**STEP)
    new_weight = weight - rate * (
        fixed_first / (jnp.sqrt(fixed_second) + ADAM_EPS) + decay_rate * weight
    )
    return (new_first, new_second, new_weight)


def mod_back(grad_hidden, ln_values, normed, scale_part, gain):
    grad_shift = jnp.sum(grad_hidden, axis=1)
    grad_scale = jnp.sum(grad_hidden * ln_values, axis=1)
    grad_ln = grad_hidden * (1.0 + scale_part)
    grad_gain = jnp.sum(grad_ln * normed, axis=(0, 1))
    return (grad_shift, grad_scale, grad_gain, grad_ln * gain)


def plain(
    tokens_in,
    cotangent,
    timesteps,
    span_start,
    span_len,
    vectors,
    w_ada,
    w_qkv,
    w_attn,
    w_in,
    w_out,
    m_vec,
    v_vec,
    m_ada,
    v_ada,
    m_qkv,
    v_qkv,
    m_attn,
    v_attn,
    m_in,
    v_in,
    m_out,
    v_out,
):
    seqs, group, width = tokens_in.shape
    heads = width // HD
    factor = HD ** (-0.5)
    flat_rows = seqs * group
    full_ada, full_qkv, full_attn, full_in, full_out = (
        lax.all_gather(w_ada.astype(jnp.bfloat16), ("dp", "seq"), axis=1, tiled=True),
        lax.all_gather(w_qkv.astype(jnp.bfloat16), ("dp", "seq"), axis=0, tiled=True),
        lax.all_gather(w_attn.astype(jnp.bfloat16), ("dp", "seq"), axis=0, tiled=True),
        lax.all_gather(w_in.astype(jnp.bfloat16), ("dp", "seq"), axis=0, tiled=True),
        lax.all_gather(w_out.astype(jnp.bfloat16), ("dp", "seq"), axis=0, tiled=True),
    )
    positions = lax.axis_index("seq") * group + jnp.arange(group, dtype=jnp.int32)
    masked = (positions[None, :] >= span_start[:, None]) & (
        positions[None, :] < (span_start + span_len)[:, None]
    )
    cond_bf = cond_input(timesteps).astype(jnp.bfloat16)
    modulation = jnp.dot(cond_bf, full_ada, preferred_element_type=jnp.float32) + vectors[
        2:8
    ].reshape(1, 6 * width)
    pieces = [modulation[:, which * width : (which + 1) * width][:, None, :] for which in range(6)]
    shift_one, scale_one, gate_one, shift_two, scale_two, gate_two = pieces
    start_tokens = jnp.where(
        masked[..., None], vectors[8][None, None, :], tokens_in.astype(jnp.float32)
    )
    normed_one, inv_one = normalize(start_tokens)
    ln_one = normed_one * vectors[0]
    hidden_one = (
        (ln_one * (1.0 + scale_one) + shift_one).astype(jnp.bfloat16).reshape(flat_rows, width)
    )
    projected = jnp.dot(hidden_one, full_qkv, preferred_element_type=jnp.float32).reshape(
        seqs, group, 3 * width
    )
    cosines, sines = rotary_tables(positions)
    queries = rotate(projected[..., :width].reshape(seqs, group, heads, HD), cosines, sines).astype(
        jnp.bfloat16
    )
    keys_here = rotate(
        projected[..., width : 2 * width].reshape(seqs, group, heads, HD), cosines, sines
    ).astype(jnp.bfloat16)
    values_here = projected[..., 2 * width :].astype(jnp.bfloat16)
    kv_local = jnp.concatenate([keys_here.reshape(seqs, group, width), values_here], axis=-1)
    initial = (
        jnp.full((seqs, heads, group), -1e30, jnp.float32),
        jnp.zeros((seqs, heads, group), jnp.float32),
        jnp.zeros((seqs, heads, group, HD), jnp.float32),
    )
    running, denom, accum = attend_piece(
        initial, lax.all_gather(kv_local, "seq", axis=1, tiled=True), queries, width, factor
    )
    attn_heads = accum / denom[..., None]
    logsum = running + jnp.log(denom)
    attn_rows = jnp.transpose(attn_heads, (0, 2, 1, 3)).reshape(flat_rows, width)
    attn_bf = attn_rows.astype(jnp.bfloat16)
    branch_one = jnp.dot(attn_bf, full_attn, preferred_element_type=jnp.float32).reshape(
        seqs, group, width
    )
    mid_tokens = start_tokens + gate_one * branch_one
    normed_two, inv_two = normalize(mid_tokens)
    ln_two = normed_two * vectors[1]
    hidden_two = (
        (ln_two * (1.0 + scale_two) + shift_two).astype(jnp.bfloat16).reshape(flat_rows, width)
    )
    pre_act = jnp.dot(hidden_two, full_in, preferred_element_type=jnp.float32)
    activ, gelu_back = jax.vjp(partial(jax.nn.gelu, approximate=True), pre_act)
    activ_bf = activ.astype(jnp.bfloat16)
    branch_two = jnp.dot(activ_bf, full_out, preferred_element_type=jnp.float32).reshape(
        seqs, group, width
    )
    block_out = (mid_tokens + gate_two * branch_two).astype(jnp.bfloat16)
    grad_y = cotangent.astype(jnp.float32)
    grad_gate_two = jnp.sum(grad_y * branch_two, axis=1)
    grad_branch_two = (grad_y * gate_two).astype(jnp.bfloat16).reshape(flat_rows, width)
    grad_w_out = jnp.dot(activ_bf.T, grad_branch_two, preferred_element_type=jnp.float32)
    grad_activ = jnp.dot(grad_branch_two, full_out.T, preferred_element_type=jnp.float32)
    grad_pre = gelu_back(grad_activ)[0].astype(jnp.bfloat16)
    grad_w_in = jnp.dot(hidden_two.T, grad_pre, preferred_element_type=jnp.float32)
    grad_hidden_two = jnp.dot(grad_pre, full_in.T, preferred_element_type=jnp.float32).reshape(
        seqs, group, width
    )
    grad_shift_two, grad_scale_two, grad_gain_two, grad_normed_two = mod_back(
        grad_hidden_two, ln_two, normed_two, scale_two, vectors[1]
    )
    grad_mid = grad_y + norm_back(normed_two, inv_two, grad_normed_two)
    grad_gate_one = jnp.sum(grad_mid * branch_one, axis=1)
    grad_branch_one = (grad_mid * gate_one).astype(jnp.bfloat16).reshape(flat_rows, width)
    grad_w_attn = jnp.dot(attn_bf.T, grad_branch_one, preferred_element_type=jnp.float32)
    grad_attn_bf = (
        jnp.dot(grad_branch_one, full_attn.T, preferred_element_type=jnp.float32)
        .astype(jnp.bfloat16)
        .reshape(seqs, group, heads, HD)
    )
    delta = jnp.einsum("sqhd,shqd->shq", grad_attn_bf.astype(jnp.float32), attn_heads)
    kv_all = lax.all_gather(kv_local, "seq", axis=1, tiled=True)
    grad_queries = query_grads(kv_all, queries, grad_attn_bf, logsum, delta, width, factor)
    grad_kv = jnp.transpose(
        lax.psum_scatter(
            key_grads(
                kv_all,
                queries,
                grad_attn_bf,
                logsum,
                delta,
                width,
                factor,
                group * lax.axis_size("seq"),
            ).astype(jnp.bfloat16),
            "seq",
            scatter_dimension=0,
            tiled=True,
        ).astype(jnp.float32),
        (1, 0, 2),
    )
    grad_keys = grad_kv[..., :width].reshape(seqs, group, heads, HD)
    grad_qkv = jnp.concatenate(
        [
            rotate_back(grad_queries, cosines, sines).reshape(seqs, group, width),
            rotate_back(grad_keys, cosines, sines).reshape(seqs, group, width),
            grad_kv[..., width:],
        ],
        axis=-1,
    )
    grad_qkv = grad_qkv.astype(jnp.bfloat16).reshape(flat_rows, 3 * width)
    grad_w_qkv = jnp.dot(hidden_one.T, grad_qkv, preferred_element_type=jnp.float32)
    grad_hidden_one = jnp.dot(grad_qkv, full_qkv.T, preferred_element_type=jnp.float32).reshape(
        seqs, group, width
    )
    grad_shift_one, grad_scale_one, grad_gain_one, grad_normed_one = mod_back(
        grad_hidden_one, ln_one, normed_one, scale_one, vectors[0]
    )
    grad_start = grad_mid + norm_back(normed_one, inv_one, grad_normed_one)
    grad_mask_row = jnp.sum(jnp.where(masked[..., None], grad_start, 0.0), axis=(0, 1))
    grad_input = jnp.where(masked[..., None], 0.0, grad_start)
    grad_mod = jnp.concatenate(
        [
            grad_shift_one,
            grad_scale_one,
            grad_gate_one,
            grad_shift_two,
            grad_scale_two,
            grad_gate_two,
        ],
        axis=1,
    )
    grad_w_ada = jnp.dot(cond_bf.astype(jnp.float32).T, grad_mod, precision=lax.Precision.HIGHEST)
    grad_vectors = jnp.concatenate(
        [
            grad_gain_one[None, :],
            grad_gain_two[None, :],
            jnp.sum(grad_mod, axis=0).reshape(6, width),
            grad_mask_row[None, :],
        ],
        axis=0,
    )
    red_ada, red_qkv, red_attn, red_in, red_out, red_vec = (
        lax.psum_scatter(grad_w_ada, ("dp", "seq"), scatter_dimension=1, tiled=True),
        lax.psum_scatter(grad_w_qkv, ("dp", "seq"), scatter_dimension=0, tiled=True),
        lax.psum_scatter(grad_w_attn, ("dp", "seq"), scatter_dimension=0, tiled=True),
        lax.psum_scatter(grad_w_in, ("dp", "seq"), scatter_dimension=0, tiled=True),
        lax.psum_scatter(grad_w_out, ("dp", "seq"), scatter_dimension=0, tiled=True),
        lax.psum_scatter(grad_vectors, ("dp", "seq"), scatter_dimension=1, tiled=True),
    )
    local_squares = jnp.float32(0.0)
    for reduced in (red_vec, red_ada, red_qkv, red_attn, red_in, red_out):
        local_squares = local_squares + jnp.sum(reduced * reduced)
    grad_norm = jnp.sqrt(lax.psum(local_squares, ("dp", "seq")))
    clip_factor = jnp.minimum(1.0, CLIP / (grad_norm + 1e-06))
    columns = red_vec.shape[1]
    own_vectors = lax.dynamic_slice_in_dim(
        vectors, lax.axis_index(("dp", "seq")) * columns, columns, 1
    )
    vec_out = adam_step(own_vectors, red_vec * clip_factor, m_vec, v_vec, RATE_VECTORS, 0.0)
    ada_out = adam_step(w_ada, red_ada * clip_factor, m_ada, v_ada, RATE, DECAY)
    qkv_out = adam_step(w_qkv, red_qkv * clip_factor, m_qkv, v_qkv, RATE, DECAY)
    attn_out = adam_step(w_attn, red_attn * clip_factor, m_attn, v_attn, RATE, DECAY)
    in_out = adam_step(w_in, red_in * clip_factor, m_in, v_in, RATE, DECAY)
    out_out = adam_step(w_out, red_out * clip_factor, m_out, v_out, RATE, DECAY)
    return (
        block_out,
        grad_input,
        grad_norm,
        vec_out[0],
        vec_out[1],
        vec_out[2],
        ada_out[0],
        ada_out[1],
        ada_out[2],
        qkv_out[0],
        qkv_out[1],
        qkv_out[2],
        attn_out[0],
        attn_out[1],
        attn_out[2],
        in_out[0],
        in_out[1],
        in_out[2],
        out_out[0],
        out_out[1],
        out_out[2],
    )


F32, BF = jnp.float32, jnp.bfloat16
MESH = pl.DeviceIdType.MESH
DP, LINE, SEQ, CHIPS, ALL = 4, 4, 8, 16, 32
ROWS, WIDTH, PACK = 128, 768, 640
HALF = WIDTH // 2
HALVES = ((0, 0), (0, 1), (0, 2), (2, 2), (1, 0), (1, 1), (1, 2), None, (2, 0), (2, 1))

def numbered(**counts):
    at = {}
    for name, count in counts.items():
        at[name] = sum(counts[other] for other in at)
    return SimpleNamespace(**at), sum(counts.values())


S, SEM_COUNT = numbered(
    load=11,
    cond=1,
    mix_qkv=1,
    mix_in=1,
    mix_attn=1,
    mod=1,
    mod_pair=1,
    w_qkv=1,
    w_attn=4,
    plane_in=1,
    w_in=4,
    w_out=4,
    group_qkv=4,
    group_attn=4,
    fw_qkv=1,
    fw_attn=1,
    fw_in=1,
    fw_out=1,
    tok=4,
    h2=4,
    dm=4,
    xf=4,
    o=1,
    mm=1,
    dh2=1,
    do=1,
    gp=1,
    dh1=5,
    pair_out=1,
    pair_in=1,
    pair_attn=1,
    pair_qkv=1,
    plane_attn=1,
    plane_qkv=1,
    line_out=5,
    line_in=5,
    slice_in=1,
    line_attn=5,
    line_qkv=1,
    last_in=1,
    last_attn=1,
    last_qkv=1,
    early=7,
    late=7,
    sq=1,
)

SCRATCH = dict(
    i_tok=((1, 128, 768), BF),
    i_cot=((1, 128, 768), BF),
    i_vec=((9, 768), F32),
    i_wada=((144, 128), F32),
    i_wqkv=((24, 2304), F32),
    i_wattn=((24, 768), F32),
    i_win=((24, 3072), F32),
    i_wout=((96, 768), F32),
    wide_qkv=((48, 3072), F32),
    wide_in=((48, 3072), F32),
    wide_attn=((48, 768), F32),
    s_qkv=((48, 3072), BF),
    s_in=((48, 3072), BF),
    s_attn=((48, 768), BF),
    w_qkv=((768, 768), BF),
    w_in=((4, 4, 48, 768), BF),
    w_attn=((768, 768), BF),
    w_out=((4, 2, 96, 768), BF),
    t_w_qkv=((640, 768), BF),
    t_w_attn=((768, 1024), BF),
    t_w_in=((768, 768), BF),
    t_w_out=((768, 768), BF),
    t_h1=((768, 512), BF),
    conds_all=((4, 8, 128), F32),
    mod_send=((4, 4, 128), F32),
    mod_got=((2, 16, 4, 128), F32),
    mod_flat=((40, 128), F32),
    mod_pad=((8, 384), F32),
    turn=((2, 4, 128, 128), F32),
    dmod_flat=((4, 40, 128), F32),
    mod=((8, 768), F32),
    x0=((128, 768), F32),
    n1=((4, 128, 768), F32),
    inv1=((4, 128, 128), F32),
    x1=((128, 768), F32),
    n2=((128, 768), F32),
    inv2=((128, 128), F32),
    a=((128, 768), F32),
    dx1=((128, 768), F32),
    toks=((4, 128, 768), BF),
    h1=((4, 128, 768), BF),
    h2=((4, 128, 768), BF),
    dm=((4, 128, 768), BF),
    gb=((4, 128, 768), BF),
    du=((4, 128, 768), BF),
    xb=((2, 4, 128, 640), BF),
    pt=((3, 1024, 512), BF),
    vt=((2, 128, 1024), BF),
    kt=((2, 128, 1024), BF),
    back=((4, 128, 768), F32),
    ot=((2, 128, 512), F32),
    os=((4, 192, 128), BF),
    ob=((4, 192, 128), BF),
    o2=((4, 128, 128), BF),
    mms=((4, 128, 768), BF),
    mmr=((4, 128, 768), BF),
    dhs=((4, 128, 768), BF),
    dhr=((4, 128, 768), BF),
    das=((128, 768), BF),
    dos=((4, 192, 128), BF),
    dob=((4, 192, 128), BF),
    dst=((3, 1024, 512), BF),
    ga=((512, 640), F32),
    gps=((512, 512), BF),
    gpr=((512, 512), BF),
    dqkv=((4, 128, 768), BF),
    d1s=((4, 128, 768), BF),
    d1r=((4, 128, 768), BF),
    g_out=((4, 2, 96, 768), BF),
    g_in=((2, 4, 4, 48, 384), BF),
    g_attn=((2, 768, 384), BF),
    g_qkv=((2, 768, 384), BF),
    p_out=((4, 96, 768), BF),
    p_in=((4, 4, 48, 384), BF),
    p_attn=((768, 384), BF),
    p_qkv=((768, 384), BF),
    q_attn=((4, 192, 384), BF),
    q_qkv=((4, 192, 384), BF),
    m_attn=((192, 384), BF),
    via_attn=((48, 384), BF),
    m_qkv=((192, 384), BF),
    r_out=((4, 96, 768), BF),
    r_in=((4, 4, 48, 384), BF),
    via_in=((4, 48, 384), BF),
    via_out=((96, 768), BF),
    via_dh1=((128, 768), BF),
    m_in=((4, 48, 384), BF),
    u_in=((4, 48, 384), BF),
    r_attn=((4, 48, 384), BF),
    r_qkv=((4, 48, 384), BF),
    t_in=((4, 48, 384), F32),
    t_attn=((1, 48, 384), F32),
    t_qkv=((4, 48, 384), F32),
    f_in=((4, 2, 24, 384), F32),
    f_attn=((1, 2, 24, 384), F32),
    f_qkv=((4, 2, 24, 384), F32),
    early=((8, 768), F32),
    early_pair=((8, 768), F32),
    early_line=((4, 8, 384), F32),
    early_plane=((4, 8, 384), F32),
    early_all=((2, 4, 8, 384), F32),
    late=((4, 768), F32),
    late_pair=((4, 768), F32),
    late_line=((4, 4, 384), F32),
    late_plane=((4, 4, 384), F32),
    late_all=((2, 4, 4, 384), F32),
    sq=((32, 1, 128), F32),
)


def dot(left, right):
    return jnp.dot(left, right, preferred_element_type=F32)


def dot_nt(left, right):
    return lax.dot_general(left, right, (((1,), (1,)), ((), ())), preferred_element_type=F32)


def dot_tn(left, right):
    return lax.dot_general(left, right, (((0,), (0,)), ((), ())), preferred_element_type=F32)


def loop(count, body, start=0):
    def step(index, carry):
        body(index)
        return carry

    lax.fori_loop(start, count, step, 0)


def layer_kernel(
    i_time,
    i_start,
    i_len,
    h_tok,
    h_cot,
    h_vec,
    h_wada,
    h_wqkv,
    h_wattn,
    h_win,
    h_wout,
    o_y,
    o_dx,
    o_norm,
    o_gqkv,
    o_gattn,
    o_gin,
    o_gout,
    o_dmod,
    o_gvec,
    o_vec,
    o_conds,
    *scratch,
):
    r = SimpleNamespace(**dict(zip(SCRATCH, scratch)), when=scratch[-3])
    send_sems, recv_sems = scratch[-2:]
    i_tok, i_cot, i_vec, i_wada = r.i_tok, r.i_cot, r.i_vec, r.i_wada
    i_wqkv, i_wattn, i_win, i_wout = r.i_wqkv, r.i_wattn, r.i_win, r.i_wout
    b, s = lax.axis_index("dp"), lax.axis_index("seq")
    z, c = lax.div(s, 2), lax.rem(s, 2)
    mate = s + 1 - 2 * c
    chip = b * LINE + z
    me = b * SEQ + s
    drains = []

    def push(src, dst, at, to_b, to_s, out=None):
        pltpu.make_async_remote_copy(
            src_ref=src,
            dst_ref=dst,
            send_sem=send_sems.at[at if out is None else out],
            recv_sem=recv_sems.at[at],
            device_id=(to_b, to_s),
            device_id_type=MESH,
        ).start()

    def keep(src, dst, at):
        pltpu.make_async_copy(src, dst, recv_sems.at[at]).start()

    def got(at, like):
        pltpu.make_async_copy(like, like, recv_sems.at[at]).wait()

    def left(at, like):
        pltpu.make_async_copy(like, like, send_sems.at[at]).wait()

    def sent(at, like):
        drains.append(lambda: left(at, like))

    def by_core(body):
        for h, width in ((0, HALF), (1, PACK - HALF)):

            @pl.when(c == h)
            def _():
                body(slice(HALF * h, HALF * h + width), width)

    def sent_by_core(at, like):
        drains.append(lambda: by_core(lambda columns, width: left(at, like(width))))

    near = (b, b + 1 - 2 * lax.rem(b, 2), b + 2 - 4 * lax.div(b, 2), 3 - b)

    def toward(k):
        if k == 3:
            return 3, near[3]
        slot = 1 + c if k == 1 else 2 - c
        return slot, (1 - c) * near[k] + c * near[3 - k]

    def peers(body):
        for k in (1, 2, 3):
            body(*toward(k))

    def stack(body):
        for k in (1, 2, 3):
            body(lax.rem(z + k + 2 * c * (2 - k), LINE))

    def line_gather(block, at, near=True, rest=True):
        inner = 1 + lax.rem(z, 2)
        if near:
            push(block(z), block(z), at + z, b, 2 * inner + c, at)

        def one(to):
            relayed = ((z == 1) & (to == 3)) | ((z == 2) & (to == 0))

            @pl.when(jnp.logical_not(relayed | (to == inner)))
            def _():
                push(block(z), block(z), at + z, b, 2 * to + c, at)

        if rest:
            stack(one)

    def line_relay(block, at):
        for middle, source, to in ((2, 1, 3), (1, 2, 0)):

            @pl.when(z == middle)
            def _():
                got(at + source, block(source))
                push(block(source), block(source), at + source, b, 2 * to + c, at)

    def line_got(block, at, k):
        here = (k == z) | ((z == 2) & (k == 1)) | ((z == 1) & (k == 2))

        @pl.when(jnp.logical_not(here))
        def _():
            got(at + k, block(0))

    far = lax.div(z, 2)

    def line_order(j):
        return lax.rem(z + (2, 3 - 2 * far, 1 + 2 * far, 0)[j], LINE)

    def line_add(j, rows, dst, via, at):
        to = line_order(j)
        outer_chip = (z == 0) | (z == 3)

        def direct():
            push(rows(to), dst.at[z], at + z, b, 2 * to + c, at)

        if j == 0:

            @pl.when(outer_chip)
            def _():
                push(rows(to), via, at + 4, b, 2 * (1 + far) + c, at)

            @pl.when(jnp.logical_not(outer_chip))
            def _():
                direct()

        elif j < 3:
            direct()
        else:
            keep(rows(z), dst.at[z], at + z)

    def line_via(via, at, add):
        @pl.when((z == 1) | (z == 2))
        def _():
            got(at + 4, via)
            add()

    def line_done(dst, at):
        for k in range(4):
            missing = ((z == 1) & (k == 3)) | ((z == 2) & (k == 0))

            @pl.when(jnp.logical_not(missing))
            def _():
                got(at + k, dst.at[k])

    def line_clear(dst):
        for middle, k in ((1, 3), (2, 0)):

            @pl.when(z == middle)
            def _():
                dst[k] = jnp.zeros(dst.shape[1:], BF)

    lane = lax.broadcasted_iota(jnp.int32, (1, 128), 1)
    low = lane < 64
    own24 = pl.ds(pl.multiple_of(24 * c, 8), 24)
    mate24 = pl.ds(pl.multiple_of(24 * (1 - c), 8), 24)
    part = pl.ds(pl.multiple_of(HALF * c, 128), HALF)
    chip_rows = pl.ds(pl.multiple_of(48 * chip, 16), 48)
    group_rows = pl.ds(pl.multiple_of(192 * b, 16), 192)

    barrier = pltpu.get_barrier_semaphore()

    def greet(k):
        other = lax.rem(me + k, ALL)
        pl.semaphore_signal(
            barrier, inc=1, device_id=(lax.div(other, SEQ), lax.rem(other, SEQ)), device_id_type=MESH
        )

    loads = (
        (i_time, r.when.at[0]),
        (i_start, r.when.at[1]),
        (i_len, r.when.at[2]),
        (h_wqkv, i_wqkv),
        (h_win, i_win),
        (h_wattn, i_wattn),
        (h_wout, i_wout),
        (h_tok, i_tok),
        (h_vec, i_vec),
        (h_wada, i_wada),
        (h_cot, i_cot),
    )
    for k, (src, dst) in enumerate(loads):
        pltpu.make_async_copy(src, dst, recv_sems.at[S.load + k]).start()
    loop(ALL, greet, 1)
    for k, (src, dst) in enumerate(loads):
        pltpu.make_async_copy(src, dst, recv_sems.at[S.load + k]).wait()

    def natural(kind, p, head):
        return kind * WIDTH + 192 * p + 64 * head

    def half_at(ref, column, high):
        tile = ref[:, column // 128 * 128 : column // 128 * 128 + 128]
        return tile if (column % 128 == 64) == high else pltpu.roll(tile, 64, 1)

    for p in range(4):
        for tile in range(5):
            pair = []
            for high in (0, 1):
                which = HALVES[2 * tile + high]
                pair.append(
                    jnp.zeros((24, 128), F32)
                    if which is None
                    else half_at(i_wqkv, natural(which[0], p, which[1]), bool(high))
                )
            r.wide_qkv[own24, 768 * p + 128 * tile : 768 * p + 128 * tile + 128] = jnp.where(
                low, pair[0], pair[1]
            )
        r.wide_qkv[own24, 768 * p + 640 : 768 * p + 768] = jnp.zeros((24, 128), F32)
    r.wide_in[own24, :] = i_win[...]
    r.wide_attn[own24, :] = i_wattn[...]
    r.w_out[z, c] = i_wout[...].astype(BF)
    r.toks[z] = i_tok[0]
    line_clear(r.r_out)
    line_clear(r.r_in)
    line_clear(r.d1r)
    line_clear(r.r_attn)
    for ref in (r.q_qkv, r.r_qkv):
        ref[:, :, PACK - HALF : HALF] = jnp.zeros((4, ref.shape[1], WIDTH - PACK), BF)
    lanes8 = lax.broadcasted_iota(jnp.int32, (8, 128), 1)
    half_cond = COND // 2
    speed = jnp.exp((lanes8 % half_cond).astype(F32) * (-math.log(10000.0) / half_cond))
    angle = r.when[0, 0].astype(F32) * speed
    wave = jnp.where(lanes8 < half_cond, jnp.cos(angle), jnp.sin(angle))
    r.conds_all[b] = wave * (1.0 / (1.0 + jnp.exp(-wave)))
    pl.semaphore_wait(barrier, ALL - 1)

    def token_block(k):
        return r.toks.at[k]

    def attn_block(k):
        return r.w_attn.at[pl.ds(pl.multiple_of(192 * b + 48 * k, 16), 48), part]

    def in_block(k):
        return r.w_in.at[:, k, :, part]

    def out_block(k):
        return r.w_out.at[k, c]

    peers(lambda k, to: push(r.conds_all.at[b], r.conds_all.at[b], S.cond, to, s))
    sent(S.cond, r.conds_all.at[0:3])
    push(r.wide_qkv.at[own24], r.wide_qkv.at[own24], S.mix_qkv, b, mate)
    sent(S.mix_qkv, r.wide_qkv.at[0:24])
    push(r.wide_attn.at[own24], r.wide_attn.at[own24], S.mix_attn, b, mate)
    sent(S.mix_attn, r.wide_attn.at[0:24])
    push(r.wide_in.at[own24], r.wide_in.at[own24], S.mix_in, b, mate)
    sent(S.mix_in, r.wide_in.at[0:24])

    line_gather(out_block, S.w_out, rest=False)

    got(S.cond, r.conds_all.at[0:3])
    row8 = lax.broadcasted_iota(jnp.int32, (8, 128), 0)
    cond4 = jnp.zeros((8, 128), F32)
    for k in range(4):
        cond4 = jnp.where(row8 == k, r.conds_all[k], cond4)
    o_conds[...] = cond4
    wide = i_wada.shape[0]
    r.mod_pad[...] = jnp.zeros((8, 384), F32)
    r.mod_pad[:, 0:wide] = dot_nt(cond4.astype(BF), i_wada[...].astype(BF))
    columns = pltpu.roll(r.mod_pad[...], lax.rem(wide * me, 128), 1)
    for k in range(4):
        for t in range(3):
            r.mod_send[k, t : t + 1, :] = columns[k : k + 1, 128 * t : 128 * t + 128]
        r.mod_send[k, 3:4, :] = jnp.zeros((1, 128), F32)

    def send_mod(k):
        other = lax.rem(chip + k, CHIPS)
        ob = lax.div(other, LINE)
        push(r.mod_send.at[ob], r.mod_got.at[c, chip], S.mod, ob, 2 * lax.rem(other, LINE) + c)

    loop(CHIPS, send_mod, 1)
    sent(S.mod, r.mod_got.at[0, 0:15])
    keep(r.mod_send.at[b], r.mod_got.at[c, chip], S.mod)

    def block(src, first):
        return src.at[:, pl.ds(pl.multiple_of(first, 128), HALF)]

    def slices_along_line():
        def send(columns, width):
            def rows(to):
                first = pl.multiple_of(WIDTH * to + columns.start, 128)
                return r.s_qkv.at[:, pl.ds(first, width)]

            dst = r.w_qkv.at[chip_rows, columns]
            stack(lambda to: push(rows(to), dst, S.w_qkv, b, 2 * to + c))
            keep(rows(z), dst, S.w_qkv)

        by_core(send)
        sent_by_core(S.w_qkv, lambda width: r.w_qkv.at[0:144, 0:width])

    def over_plane(dst, at):
        rows = dst.at[group_rows, part]
        peers(lambda k, to: push(rows, rows, at + k, to, s))
        for k in (1, 2, 3):
            sent(at + k, dst.at[0:192, 0:HALF])

    def share(dst, at, onward):
        for k in range(4):
            rows = dst.at[pl.ds(pl.multiple_of(192 * near[k], 16), 192), part]
            if k:
                got(at + k, rows)
            push(rows, rows, onward, b, mate)
        sent(onward, dst.at[:, 0:HALF])

    def line_share(block, at, onward):
        for k in range(4):
            line_got(block, at, k)
            push(block(k), block(k), onward, b, mate)

    got(S.mix_qkv, r.wide_qkv.at[0:24])
    r.s_qkv[...] = r.wide_qkv[...].astype(BF)
    slices_along_line()
    line_gather(token_block, S.tok, rest=False)
    sent(S.tok, r.toks.at[0:3])
    got(S.mix_attn, r.wide_attn.at[0:24])
    r.s_attn[...] = r.wide_attn[...].astype(BF)

    def qkv_over_plane(columns, width):
        got(S.w_qkv, r.w_qkv.at[0:192, 0:width])
        rows = r.w_qkv.at[group_rows, columns]
        peers(lambda k, to: push(rows, rows, S.group_qkv + k, to, s))

    by_core(qkv_over_plane)
    for k in (1, 2, 3):
        sent_by_core(S.group_qkv + k, lambda width: r.w_qkv.at[0:192, 0:width])
    line_gather(token_block, S.tok, near=False)
    for h in range(2):

        @pl.when(c == h)
        def _():
            r.w_attn[chip_rows, 384 * h : 384 * h + 384] = r.s_attn[:, 384 * h : 384 * h + 384]

    line_gather(attn_block, S.w_attn)
    sent(S.w_attn, r.w_attn.at[0:144, 0:HALF])
    line_gather(out_block, S.w_out, near=False)
    sent(S.w_out, r.w_out.at[0:3, 0])
    got(S.mix_in, r.wide_in.at[0:24])
    r.s_in[...] = r.wide_in[...].astype(BF)
    peers(
        lambda k, to: push(
            block(r.s_in, WIDTH * to + HALF * c), r.w_in.at[b, z, :, part], S.plane_in, to, s
        )
    )
    keep(block(r.s_in, WIDTH * b + HALF * c), r.w_in.at[b, z, :, part], S.plane_in)
    sent(S.plane_in, r.w_in.at[0:3, 0, :, 0:HALF])

    def hidden_rows(k):
        place = (2 * k + c) * ROWS + lax.broadcasted_iota(jnp.int32, (ROWS, 1), 0)
        return (place >= r.when[1, 0]) & (place < r.when[1, 0] + r.when[2, 0])

    def first_norm(tokens, k):
        x0 = jnp.where(hidden_rows(k), i_vec[8:9, :], tokens.astype(F32))
        normed, inverse = normalize(x0)
        r.n1[k] = normed
        r.inv1[k] = jnp.broadcast_to(inverse, (ROWS, 128))
        return x0

    r.x0[...] = first_norm(i_tok[0], z)

    got(S.mod, r.mod_got.at[0])
    push(r.mod_got.at[c], r.mod_got.at[c], S.mod_pair, b, mate)
    sent(S.mod_pair, r.mod_got.at[0])
    got(S.mod_pair, r.mod_got.at[0])
    r.mod_flat[...] = jnp.zeros((40, 128), F32)
    for k in range(ALL):
        first = 9 * k // 8
        r.mod_flat[first : first + 3, :] += r.mod_got[k % 2, k // 2, 0:3, :]
    for k in range(6):
        row = jnp.concatenate(
            [r.mod_flat[6 * k + t : 6 * k + t + 1, :] for t in range(6)], axis=1
        )
        r.mod[k : k + 1, :] = row + i_vec[2 + k : 3 + k, :]

    def mod(k):
        return r.mod[k : k + 1, :]

    def vec(k):
        return i_vec[k : k + 1, :]

    r.h1[z] = (r.n1[z] * vec(0) * (1.0 + mod(1)) + mod(0)).astype(BF)
    r.dm[0] = (i_cot[0].astype(F32) * mod(5)).astype(BF)
    peers(lambda k, to: push(r.dm.at[0], r.dm.at[k], S.dm + k, to, s))
    for k in (1, 2, 3):
        sent(S.dm + k, r.dm.at[0])

    lanes = lax.broadcasted_iota(jnp.int32, (ROWS, 128), 1)
    first_half = lanes % HD < HD // 2
    speed = jnp.exp((lanes % (HD // 2)).astype(F32) * (-math.log(10000.0) / (HD // 2)))
    row = lax.broadcasted_iota(jnp.int32, (ROWS, 128), 0)

    def table(k):
        angle = ((2 * k + c) * ROWS + row).astype(F32) * speed
        r.turn[0, k] = jnp.cos(angle)
        sine = jnp.sin(angle)
        r.turn[1, k] = jnp.where(first_half, -sine, sine)

    loop(LINE, table)

    line_relay(token_block, S.tok)

    def qkv_share(columns, width):
        for k in range(4):
            rows = r.w_qkv.at[pl.ds(pl.multiple_of(192 * near[k], 16), 192), columns]
            if k:
                got(S.group_qkv + k, rows)
            push(rows, rows, S.fw_qkv, b, mate)

    by_core(qkv_share)
    sent_by_core(S.fw_qkv, lambda width: r.w_qkv.at[:, 0:width])
    by_core(lambda columns, width: got(S.fw_qkv, r.w_qkv.at[:, 0 : PACK - width]))
    for k in range(5):
        columns = slice(128 * k, 128 * k + 128)
        r.t_w_qkv[columns, :] = r.w_qkv[:, columns].T

    def turned(tile, sign, k):
        other = jnp.where(first_half, pltpu.roll(tile, 96, 1), pltpu.roll(tile, 32, 1))
        return tile * r.turn[0, k] + sign * (other * r.turn[1, k])

    def project(j):
        k = lax.rem(z + j, LINE)

        @pl.when(j > 0)
        def _():
            line_got(token_block, S.tok, k)
            first_norm(r.toks[k], k)
            r.h1[k] = (r.n1[k] * vec(0) * (1.0 + mod(1)) + mod(0)).astype(BF)

        x = dot(r.h1[k], r.w_qkv[:, 0:PACK])
        tiles = [x[:, 128 * t : 128 * t + 128] for t in range(5)]
        tiles[0] = turned(tiles[0], 1.0, k) * 0.125
        tiles[1] = jnp.where(low, turned(tiles[1], 1.0, k) * 0.125, tiles[1])
        tiles[2] = turned(tiles[2], 1.0, k)
        tiles[3] = turned(tiles[3], 1.0, k)
        for t in range(5):
            r.xb[0, k, :, 128 * t : 128 * t + 128] = tiles[t].astype(BF)
        push(r.xb.at[0, k], r.xb.at[1, k], S.xf + k, b, mate)

    loop(4, project)
    line_relay(attn_block, S.w_attn)
    for k in range(4):
        line_got(attn_block, S.w_attn, k)
    over_plane(r.w_attn, S.group_attn)
    for k in range(4):
        sent(S.xf + k, r.xb.at[0, 0])

    for k in range(6):
        columns = slice(128 * k, 128 * k + 128)
        r.t_h1[columns, :] = r.h1[:, :, columns].reshape(512, 128).T
    for k in range(4):
        got(S.xf + k, r.xb.at[0, 0])

    def tile_of(t):
        return r.xb[:, :, :, 128 * t : 128 * t + 128].reshape(1024, 128)

    heads = ((0, 2, 4, True, True), (0, 2, 4, False, False), (1, 3, 1, True, False))

    def queries(head, first, size):
        q_tile, _, _, q_low, _ = heads[head]
        q = r.xb[0, first : first + size, :, 128 * q_tile : 128 * q_tile + 128]
        return jnp.where(low if q_low else ~low, q.reshape(size * 128, 128), jnp.zeros((), BF))

    r.vt[0] = tile_of(4).T
    r.vt[1] = tile_of(1).T
    for half in range(2):
        at = slice(256 * half, 256 * half + 256)
        for head in range(3):
            scores = dot_nt(tile_of(heads[head][1]), queries(head, 2 * half, 2))
            weights = jnp.exp(scores - jnp.max(scores, axis=0, keepdims=True))
            weights = weights * (1.0 / jnp.sum(weights, axis=0, keepdims=True))
            weights = weights.astype(BF)
            r.pt[head, :, at] = weights
            out = dot(r.vt[head // 2], weights)
            if head == 0:
                r.ot[0, 0:64, at] = out[0:64]
            elif head == 1:
                r.ot[0, 64:128, at] = out[64:128]
            else:
                r.ot[1, 0:64, at] = out[64:128]
                r.ot[1, 64:128, at] = jnp.zeros((64, 256), F32)
        for k in (2 * half, 2 * half + 1):
            across = slice(128 * k, 128 * k + 128)
            r.os[k, 0:128, :] = r.ot[0, :, across].T.astype(BF)
            third = r.ot[1, 0:64, across]
            third = jnp.concatenate([third, pltpu.roll(third, 64, 1)], axis=0)
            r.os[k, 128:192, :] = third.T[0:64].astype(BF)
        for to in (2 * half, 2 * half + 1):

            @pl.when(z == to)
            def _():
                keep(r.os.at[to], r.ob.at[z], S.o)

            @pl.when(z != to)
            def _():
                push(r.os.at[to], r.ob.at[z], S.o, b, 2 * to + c)

        if half == 0:
            line_relay(out_block, S.w_out)

    sent(S.o, r.os.at[0:3])
    got(S.plane_in, r.w_in.at[:, 0, :, 0:HALF])
    line_gather(in_block, S.w_in)
    sent(S.w_in, r.w_in.at[0:3, :, :, 0:HALF])
    for k in range(2):
        r.kt[k] = tile_of(2 + k).T
    share(r.w_attn, S.group_attn, S.fw_attn)
    got(S.fw_attn, r.w_attn.at[:, 0:HALF])
    for p in range(4):
        first = 192 * p
        r.t_w_attn[:, 256 * p : 256 * p + 128] = r.w_attn[first : first + 128, :].T
        third = r.w_attn[first + 128 : first + 192, :]
        r.t_w_attn[:, 256 * p + 128 : 256 * p + 256] = jnp.concatenate(
            [third, jnp.zeros_like(third)], axis=0
        ).T
    got(S.o, r.ob)
    a = jnp.zeros((ROWS, WIDTH), F32)
    for p in range(4):
        third = r.ob[p, 128:192, :].astype(F32)
        third = jnp.concatenate([third, pltpu.roll(third, 64, 1)], axis=0)
        r.o2[p] = jnp.where(low, third, 0.0).astype(BF)
        a += dot(r.ob[p, 0:128, :], r.w_attn[192 * p : 192 * p + 128, :])
        a += dot(r.o2[p, :, 0:64], r.w_attn[192 * p + 128 : 192 * p + 192, :])
    r.a[...] = a
    x1 = r.x0[...] + mod(2) * a
    r.x1[...] = x1
    n2, inv2 = normalize(x1)
    r.n2[...] = n2
    r.inv2[...] = jnp.broadcast_to(inv2, (ROWS, 128))
    r.h2[0] = (n2 * vec(1) * (1.0 + mod(4)) + mod(3)).astype(BF)
    for k in (1, 2):
        slot, to = toward(k)
        push(r.h2.at[0], r.h2.at[slot], S.h2 + slot, to, s)
    for k in (1, 2, 3):
        sent(S.h2 + k, r.h2.at[0])
    line_relay(in_block, S.w_in)
    got(S.h2 + 1 + c, r.h2.at[0])
    push(r.h2.at[1 + c], r.h2.at[3], S.h2 + 3, toward(2)[1], s)
    line_share(out_block, S.w_out, S.fw_out)
    sent(S.fw_out, r.w_out.at[:, 0])
    got(S.fw_out, r.w_out.at[:, 0])

    for k in range(6):
        columns = slice(128 * k, 128 * k + 128)
        r.t_w_out[columns, :] = r.w_out[:, :, :, columns].reshape(WIDTH, 128).T

    def feed_back(k):
        @pl.when(k > 0)
        def _():
            got(S.dm + k, r.dm.at[0])

        r.back[k] = dot(r.dm[k], r.t_w_out[...])

    loop(4, feed_back)
    line_share(in_block, S.w_in, S.fw_in)
    sent(S.fw_in, r.w_in.at[:, :, :, 0:HALF])
    got(S.fw_in, r.w_in.at[:, :, :, 0:HALF])
    for k in range(6):
        columns = slice(128 * k, 128 * k + 128)
        r.t_w_in[columns, :] = r.w_in[:, :, :, columns].reshape(WIDTH, 128).T

    def feed(first, count):
        at = slice(first, first + count)
        size = count * ROWS
        u = dot(r.h2[at].reshape(size, WIDTH), r.w_in[...].reshape(WIDTH, WIDTH))
        slope = 0.7978845608028654
        cube = 0.044715
        t = jnp.tanh(slope * (u + cube * u * u * u))
        r.gb[at] = (0.5 * u * (1.0 + t)).astype(BF).reshape(count, ROWS, WIDTH)
        bend = 0.5 * (1.0 + t) + 0.5 * u * (1.0 - t * t) * (slope * (1.0 + 3.0 * cube * u * u))
        du = (r.back[at].reshape(size, WIDTH) * bend).astype(BF)
        r.du[at] = du.reshape(count, ROWS, WIDTH)
        r.dhs[at] = dot(du, r.t_w_in[...]).astype(BF).reshape(count, ROWS, WIDTH)

    feed(0, 1)
    for first, count in ((1, 2), (3, 1)):
        got(S.h2 + (2 - c if first == 1 else 3), r.h2.at[0])
        feed(first, count)
        for k in range(first, first + count):
            slot, to = toward(k)
            push(r.dhs.at[slot], r.dhr.at[slot], S.dh2, to, s)
    sent(S.dh2, r.dhs.at[0:3])
    def gather(own, others):
        total = own[0].astype(F32)
        for k in (1, 2, 3):
            total += others[k].astype(F32)
        return total

    for k in range(2):
        rows = slice(384 * k, 384 * k + 384)
        result = dot_tn(r.gb[:, :, rows].reshape(512, 384), r.dm[...].reshape(512, 768))
        r.g_out[2 * k : 2 * k + 2] = result.astype(BF).reshape(2, 2, 96, 768)
    push(r.g_out.at[:, 1 - c], r.p_out, S.pair_out, b, mate)
    sent(S.pair_out, r.p_out)

    def to_mate(grad, dst, at):
        push(grad.at[1 - c], dst, at, b, mate)
        sent(at, dst)

    def pair_sum(grad, pair, at):
        got(at, pair)
        grad[c] = (grad[c].astype(F32) + pair[...].astype(F32)).astype(BF)

    def plane_sum(grad, dst, at, packed=False):
        def send(columns, width):
            def rows(to):
                return grad.at[c, pl.ds(pl.multiple_of(192 * to, 16), 192), 0:width]

            peers(lambda k, to: push(rows(to), dst.at[k, :, 0:width], at, to, s))
            keep(rows(b), dst.at[0, :, 0:width], at)

        if packed:
            by_core(send)
            sent_by_core(at, lambda width: dst.at[0:3, :, 0:width])
        else:
            send(None, HALF)
            sent(at, dst.at[0:3])

    def line_sum(src, total, dst, first, at, packed=False):
        def send(columns, width):
            got(first, src.at[:, :, 0:width])
            total[...] = (
                (src[0].astype(F32) + src[1].astype(F32))
                + (src[2].astype(F32) + src[3].astype(F32))
            ).astype(BF)

            def rows(to):
                return total.at[pl.ds(pl.multiple_of(48 * to, 16), 48), 0:width]

            stack(lambda to: push(rows(to), dst.at[z, :, 0:width], at, b, 2 * to + c))
            keep(rows(z), dst.at[z, :, 0:width], at)

        if packed:
            by_core(send)
            sent_by_core(at, lambda width: dst.at[0:3, :, 0:width])
        else:
            send(None, HALF)
            sent(at, dst.at[0:3])

    def trade(total, final, at):
        push(total.at[:, mate24], final.at[:, c], at, b, mate)
        sent(at, final.at[:, 0])
        final[:, c] = total[:, own24, :]

    def in_product(k):
        rows = slice(384 * k, 384 * k + 384)
        result = dot_tn(r.h2[:, :, rows].reshape(512, 384), r.du[...].reshape(512, 768)).astype(BF)
        for h in range(2):
            r.g_in[h, 2 * k : 2 * k + 2] = result[:, 384 * h : 384 * h + 384].reshape(2, 4, 48, 384)

    in_product(0)

    got(S.pair_out, r.p_out)
    for k in range(4):
        r.g_out[k, c] = (r.g_out[k, c].astype(F32) + r.p_out[k].astype(F32)).astype(BF)

    def out_rows(k):
        return r.g_out.at[k, c]

    for j in (0, 1):
        line_add(j, out_rows, r.r_out, r.via_out, S.line_out)
    in_product(1)
    to_mate(r.g_in, r.p_in, S.pair_in)

    def add_out():
        k = line_order(2)
        r.g_out[k, c] = (r.g_out[k, c].astype(F32) + r.via_out[...].astype(F32)).astype(BF)

    got(S.dh2, r.dhr.at[0:3])
    dh = gather(r.dhs, r.dhr)
    n2 = r.n2[...]
    inv2 = r.inv2[:, 0:1]
    r.early[...] = jnp.zeros((8, 768), F32)
    r.early[2:3, :] = jnp.sum(dh, axis=0, keepdims=True)
    both = jnp.sum(dh * n2, axis=0, keepdims=True)
    r.early[3:4, :] = both * vec(1)
    r.early[0:1, :] = both * (1.0 + mod(4))
    grad = dh * ((1.0 + mod(4)) * vec(1))
    dx1 = i_cot[0].astype(F32) + norm_back(n2, inv2, grad)
    r.dx1[...] = dx1
    r.early[1:2, :] = jnp.sum(dx1 * r.a[...], axis=0, keepdims=True)
    r.das[...] = (dx1 * mod(2)).astype(BF)
    def make_do(to):
        columns = pl.ds(pl.multiple_of(256 * to, 256), 256)
        result = dot(r.das[...], r.t_w_attn[:, columns])
        r.dos[to, 0:128, :] = result[:, 0:128].astype(BF)
        third = result[:, 128:256]
        third = jnp.where(low, third[0:64], pltpu.roll(third[64:128], 64, 1))
        r.dos[to, 128:192, :] = third.astype(BF)

    def send_do(to):
        make_do(to)
        push(r.dos.at[to], r.dob.at[z], S.do, b, 2 * to + c)

    stack(send_do)
    make_do(z)
    keep(r.dos.at[z], r.dob.at[z], S.do)
    sent(S.do, r.dos.at[0:3])
    for p in range(4):
        for rows, left_side in (
            (slice(192 * p, 192 * p + 128), r.ob[p, 0:128, :]),
            (slice(192 * p + 128, 192 * p + 192), r.o2[p]),
        ):
            result = dot_tn(left_side, r.das[...])[0 : rows.stop - rows.start].astype(BF)
            r.g_attn[0, rows, :] = result[:, 0:HALF]
            r.g_attn[1, rows, :] = result[:, HALF:WIDTH]
    to_mate(r.g_attn, r.p_attn, S.pair_attn)
    for t in range(3):
        at = slice(256 * t, 256 * t + 256)
        mm = dot(r.gb[...].reshape(512, WIDTH), r.w_out[:, :, :, at].reshape(WIDTH, 256))
        r.mms[:, :, at] = mm.astype(BF).reshape(4, ROWS, 256)

    def small_sum(src, pair, line, plane, whole, at):
        def first():
            push(src, pair, at, b, mate)
            sent(at, src)

        def second():
            got(at, pair)
            total = src[...] + pair[...]
            line[z] = (1 - c) * total[:, 0:HALF] + c * total[:, HALF:WIDTH]
            stack(lambda to: push(line.at[z], line.at[z], at + 1, b, 2 * to + c))
            sent(at + 1, line.at[0:3])

        def third():
            got(at + 1, line.at[0:3])
            plane[b] = (line[0] + line[1]) + (line[2] + line[3])
            peers(lambda k, to: push(plane.at[b], plane.at[b], at + 2, to, s))
            sent(at + 2, plane.at[0:3])

        def fourth():
            got(at + 2, plane.at[0:3])
            whole[c] = plane[...]
            push(plane, whole.at[c], at + 3, b, mate)
            sent(at + 3, plane)

        def rows(k):
            return jnp.concatenate([whole[0, k], whole[1, k]], axis=1)

        return first, second, third, fourth, rows

    early_steps = small_sum(
        r.early, r.early_pair, r.early_line, r.early_plane, r.early_all, S.early
    )
    late_steps = small_sum(r.late, r.late_pair, r.late_line, r.late_plane, r.late_all, S.late)

    pair_sum(r.g_in, r.p_in, S.pair_in)
    line_via(r.via_out, S.line_out, add_out)
    for j in (2, 3):
        line_add(j, out_rows, r.r_out, r.via_out, S.line_out)
    sent(S.line_out, r.r_out.at[0:3])

    def in_rows(k):
        return r.g_in.at[c, :, k]

    for j in (0, 1):
        line_add(j, in_rows, r.r_in, r.via_in, S.line_in)

    def add_in():
        k = line_order(2)
        r.g_in[c, :, k] = (r.g_in[c, :, k].astype(F32) + r.via_in[...].astype(F32)).astype(BF)

    pair_sum(r.g_attn, r.p_attn, S.pair_attn)
    plane_sum(r.g_attn, r.q_attn, S.plane_attn)
    peers(lambda k, to: push(r.mms.at[k], r.mmr.at[k], S.mm, to, s))
    sent(S.mm, r.mms.at[0:3])

    got(S.do, r.dob)
    dot0 = r.dob[:, 0:128, :].reshape(512, 128)
    third = r.dob[:, 128:192, :].astype(F32).reshape(256, 128)
    other_rows = jnp.where(low, pltpu.roll(third, 64, 1), 0.0).reshape(4, 64, 128)
    third = jnp.where(low, third, 0.0).reshape(4, 64, 128)
    dot1 = jnp.concatenate([third, other_rows], axis=1).reshape(512, 128)
    zero = jnp.zeros((), BF)
    moved = pltpu.roll(dot1, 64, 1).astype(BF)
    grads = (jnp.where(low, dot0, zero), jnp.where(low, zero, dot0), moved)
    product = dot0.astype(F32).T * r.ot[0]
    deltas = (
        jnp.sum(product[0:64], axis=0, keepdims=True),
        jnp.sum(product[64:128], axis=0, keepdims=True),
        jnp.sum(dot1.T * r.ot[1], axis=0, keepdims=True),
    )
    for head in range(3):
        values = tile_of(heads[head][2])
        for half in range(2):
            at = slice(256 * half, 256 * half + 256)
            dp = dot_nt(values, grads[head][at])
            r.dst[head, :, at] = (
                r.pt[head, :, at].astype(F32) * (dp - deltas[head][:, at])
            ).astype(BF)

    def key_grads(rows):
        dk = [dot(r.dst[head, rows, :], queries(head, 0, 4)) for head in range(3)]
        dv = [dot(r.pt[head, rows, :], grads[head]) for head in range(3)]
        return (dv[2], dk[0] + dk[1], dk[2], dv[0] + dv[1])

    line_via(r.via_in, S.line_in, add_in)
    for j in (2, 3):
        line_add(j, in_rows, r.r_in, r.via_in, S.line_in)
    sent(S.line_in, r.r_in.at[0:3])
    for t, tile in enumerate(key_grads(slice(512, 1024))):
        r.gps[:, 128 * t : 128 * t + 128] = tile.astype(BF)
    push(r.gps, r.gpr, S.gp, b, mate)
    sent(S.gp, r.gps)
    got(S.plane_attn, r.q_attn)
    r.m_attn[...] = (
        (r.q_attn[0].astype(F32) + r.q_attn[1].astype(F32))
        + (r.q_attn[2].astype(F32) + r.q_attn[3].astype(F32))
    ).astype(BF)

    def attn_rows(k):
        return r.m_attn.at[pl.ds(pl.multiple_of(48 * k, 16), 48)]

    for j in (0, 1):
        line_add(j, attn_rows, r.r_attn, r.via_attn, S.line_attn)
    for t, tile in enumerate(key_grads(slice(0, 512))):
        r.ga[:, 128 * t + 128 : 128 * t + 256] = tile
    for half in range(2):
        at = slice(256 * half, 256 * half + 256)
        turned_q = [dot(r.kt[head // 2], r.dst[head, :, at]) for head in range(3)]
        top = jnp.concatenate([turned_q[0][0:64], turned_q[1][64:128]], axis=0)
        r.ga[at, 0:128] = top.T * 0.125
        r.ga[at, 128:256] += turned_q[2].T * 0.125
    got(S.gp, r.gpr)

    def dh1_rows(k):
        return r.d1s.at[k]

    def back_turn(k):
        rows = pl.ds(pl.multiple_of(128 * k, 128), 128)
        tiles = [r.ga[rows, 0:128]] + [
            r.ga[rows, 128 * t : 128 * t + 128]
            + r.gpr[rows, 128 * t - 128 : 128 * t].astype(F32)
            for t in range(1, 5)
        ]
        tiles[0] = turned(tiles[0], -1.0, k)
        tiles[1] = jnp.where(low, turned(tiles[1], -1.0, k), tiles[1])
        tiles[2] = turned(tiles[2], -1.0, k)
        tiles[3] = turned(tiles[3], -1.0, k)
        for t in range(5):
            r.dqkv[k, :, 128 * t : 128 * t + 128] = tiles[t].astype(BF)
        r.dqkv[k, :, PACK:WIDTH] = jnp.zeros((128, 128), BF)

    def add_attn():
        rows = pl.ds(pl.multiple_of(48 * line_order(2), 16), 48)
        r.m_attn[rows, :] = (
            r.m_attn[rows, :].astype(F32) + r.via_attn[...].astype(F32)
        ).astype(BF)

    back_turn(line_order(0))

    def unproject(j):
        k = line_order(j)
        partial_sum = dot(r.dqkv[k, :, 0:PACK], r.t_w_qkv[...])
        r.d1s[k] = partial_sum.astype(BF)
        if j == 2:

            def add():
                r.d1s[k] = (partial_sum + r.via_dh1[...].astype(F32)).astype(BF)

            line_via(r.via_dh1, S.dh1, add)
        line_add(j, dh1_rows, r.d1r, r.via_dh1, S.dh1)
        n = r.n1[k]
        e = partial_sum * ((1.0 + mod(1)) * vec(0))
        weight = jnp.where(hidden_rows(k), r.inv1[k][:, 0:1], 0.0)
        centred = (
            e
            - jnp.mean(e, axis=-1, keepdims=True)
            - n * jnp.mean(e * n, axis=-1, keepdims=True)
        )
        r.late[0:1, :] += jnp.sum(partial_sum * n, axis=0, keepdims=True)
        r.late[1:2, :] += jnp.sum(partial_sum, axis=0, keepdims=True)
        r.late[3:4, :] += jnp.sum(weight * centred, axis=0, keepdims=True)

    r.late[...] = jnp.zeros((4, 768), F32)
    r.late[3:4, :] = jnp.sum(
        jnp.where(hidden_rows(z), r.dx1[...], 0.0), axis=0, keepdims=True
    )
    unproject(0)
    line_via(r.via_attn, S.line_attn, add_attn)
    for j in (2, 3):
        line_add(j, attn_rows, r.r_attn, r.via_attn, S.line_attn)
    sent(S.line_attn, r.r_attn.at[0:3])
    for j in (1, 2, 3):
        back_turn(line_order(j))

    def qkv_rows(k):
        rows = pl.ds(pl.multiple_of(128 * k, 128), 128)
        result = dot(r.t_h1[rows, :], r.dqkv[...].reshape(512, WIDTH)).astype(BF)
        r.g_qkv[0, rows, :] = result[:, 0:HALF]
        r.g_qkv[1, rows, :] = result[:, HALF:WIDTH]

    loop(6, qkv_rows)
    to_mate(r.g_qkv, r.p_qkv, S.pair_qkv)
    unproject(1)
    pair_sum(r.g_qkv, r.p_qkv, S.pair_qkv)
    plane_sum(r.g_qkv, r.q_qkv, S.plane_qkv, True)
    got(S.mm, r.mmr.at[0:3])
    mm = gather(r.mms, r.mmr)
    o_y[...] = (r.x1[...] + mod(5) * mm).astype(BF)
    r.early[4:5, :] = jnp.sum(i_cot[0].astype(F32) * mm, axis=0, keepdims=True)
    early_steps[0]()
    unproject(2)
    unproject(3)
    sent(S.dh1, r.d1s.at[0:3])
    both = r.late[0:1, :]
    r.late[2:3, :] = both * vec(0)
    r.late[0:1, :] = both * (1.0 + mod(1))
    late_steps[0]()
    early_steps[1]()
    late_steps[1]()

    line_done(r.r_in, S.line_in)
    r.m_in[...] = (
        (r.r_in[0].astype(F32) + r.r_in[1].astype(F32))
        + (r.r_in[2].astype(F32) + r.r_in[3].astype(F32))
    ).astype(BF)
    peers(lambda k, to: push(r.m_in.at[to], r.u_in.at[b], S.slice_in, to, s))
    keep(r.m_in.at[b], r.u_in.at[b], S.slice_in)
    sent(S.slice_in, r.u_in.at[0:3])
    line_sum(r.q_qkv, r.m_qkv, r.r_qkv, S.plane_qkv, S.line_qkv, True)
    early_steps[2]()
    late_steps[2]()

    line_done(r.d1r, S.dh1)
    dh = (r.d1r[0].astype(F32) + r.d1r[1].astype(F32)) + (
        r.d1r[2].astype(F32) + r.d1r[3].astype(F32)
    )
    n1 = r.n1[z]
    grad = dh * ((1.0 + mod(1)) * vec(0))
    dx0 = r.dx1[...] + norm_back(n1, r.inv1[z][:, 0:1], grad)
    o_dx[...] = jnp.where(hidden_rows(z), 0.0, dx0)
    early_steps[3]()
    late_steps[3]()

    line_done(r.r_out, S.line_out)
    total = (r.r_out[0].astype(F32) + r.r_out[1].astype(F32)) + (
        r.r_out[2].astype(F32) + r.r_out[3].astype(F32)
    )
    o_gout[...] = total
    squares = total * total
    squares = jnp.sum(squares[:, 0:128] + squares[:, 128:256] + squares[:, 256:384]
                      + squares[:, 384:512] + squares[:, 512:640] + squares[:, 640:768],
                      axis=0, keepdims=True)

    def fold(value):
        total = value[:, 0:128] * value[:, 0:128]
        for t in range(1, value.shape[1] // 128):
            total += value[:, 128 * t : 128 * t + 128] * value[:, 128 * t : 128 * t + 128]
        return jnp.sum(total, axis=0, keepdims=True)

    got(S.slice_in, r.u_in)
    r.t_in[...] = r.u_in[...].astype(F32)
    for p in range(4):
        squares += fold(r.t_in[p])
    trade(r.t_in, r.f_in, S.last_in)
    line_done(r.r_attn, S.line_attn)
    r.t_attn[0] = (r.r_attn[0].astype(F32) + r.r_attn[1].astype(F32)) + (
        r.r_attn[2].astype(F32) + r.r_attn[3].astype(F32)
    )
    squares += fold(r.t_attn[0])
    trade(r.t_attn, r.f_attn, S.last_attn)
    by_core(lambda columns, width: got(S.line_qkv, r.r_qkv.at[:, :, 0:width]))
    r.t_qkv[...] = r.r_qkv[...].astype(F32)
    trade(r.t_qkv, r.f_qkv, S.last_qkv)
    for p in range(4):
        squares += fold(r.t_qkv[p])
    r.sq[me] = squares

    def send_sq(k):
        other = lax.rem(me + k, ALL)
        push(r.sq.at[me], r.sq.at[me], S.sq, lax.div(other, SEQ), lax.rem(other, SEQ))

    loop(ALL, send_sq, 1)
    sent(S.sq, r.sq.at[0:31])
    got(S.last_in, r.f_in.at[:, 0])
    got(S.last_attn, r.f_attn.at[:, 0])
    for h in range(2):
        for p in range(4):
            value = r.f_in[p, h]
            o_gin[:, 768 * p + 384 * h : 768 * p + 384 * h + 384] = value
        value = r.f_attn[0, h]
        o_gattn[:, 384 * h : 384 * h + 384] = value
    got(S.last_qkv, r.f_qkv.at[:, 0])
    where = {which: index for index, which in enumerate(HALVES) if which is not None}

    def packed_half(chunk, high):
        kind, rest = chunk // 12, chunk % 12
        index = where[(kind, rest % 3)]
        t = index // 2
        tile = r.f_qkv[rest // 3, t // 3, :, t % 3 * 128 : t % 3 * 128 + 128]
        return tile if index % 2 == high else pltpu.roll(tile, 64, 1)

    for t in range(18):
        o_gqkv[:, 128 * t : 128 * t + 128] = jnp.where(
            low, packed_half(2 * t, 0), packed_half(2 * t + 1, 1)
        )
    got(S.early + 3, r.early_all.at[0])
    got(S.late + 3, r.late_all.at[0])
    early_rows = [early_steps[4](k) for k in range(4)]
    late_rows = [late_steps[4](k) for k in range(4)]
    mods = []
    for k in range(4):
        early, late = early_rows[k], late_rows[k]
        rows = jnp.concatenate([late[1:3], early[1:5], jnp.zeros((2, 768), F32)], axis=0)
        for n in range(6):
            for m in range(6):
                r.dmod_flat[k, 6 * n + m : 6 * n + m + 1, :] = rows[
                    n : n + 1, 128 * m : 128 * m + 128
                ]
        mods.append(rows)
    gain = jnp.concatenate(
        [
            sum(late_rows[k][0:1] for k in range(4)),
            sum(early_rows[k][0:1] for k in range(4)),
            (mods[0] + mods[1] + mods[2] + mods[3])[0:6],
        ],
        axis=0,
    )
    mask_row = sum(late_rows[k][3:4] for k in range(4))
    gains = jnp.concatenate([gain, mask_row, jnp.zeros((7, 768), F32)], axis=0)
    masters = jnp.concatenate([i_vec[...], jnp.zeros((7, 768), F32)], axis=0)
    own = lax.rem(WIDTH - 24 * me, WIDTH)
    o_gvec[...] = pltpu.roll(gains, own, 1)[:, 0:128]
    o_vec[...] = pltpu.roll(masters, own, 1)[:, 0:128]
    r.mod_pad[...] = jnp.zeros((8, 384), F32)
    window = lax.div(wide * me, 128)
    for k in range(4):
        rows = r.dmod_flat[k, pl.ds(window, 3), :]
        for m in range(3):
            r.mod_pad[k : k + 1, 128 * m : 128 * m + 128] = rows[m : m + 1, :]
    o_dmod[...] = pltpu.roll(r.mod_pad[...], lax.rem(384 - lax.rem(wide * me, 128), 384), 1)[:, 0:256]
    small = jnp.sum(gain * gain) + jnp.sum(mask_row * mask_row)
    conds = [r.conds_all[k][0:1].astype(BF).astype(F32) for k in range(4)]
    for k in range(4):
        for m in range(k, 4):
            term = jnp.sum(mods[k] * mods[m]) * jnp.sum(conds[k] * conds[m])
            small += term if m == k else 2.0 * term
    got(S.sq, r.sq.at[0:31])
    total = r.sq[0]
    for k in range(1, ALL):
        total += r.sq[k]
    o_norm[...] = jnp.broadcast_to(jnp.sqrt(jnp.sum(total) + small), (8, 128))

    for drained in drains:
        drained()


def run_layer(*args):
    shapes = (
        ((ROWS, WIDTH), BF),
        ((ROWS, WIDTH), F32),
        ((8, 128), F32),
        ((24, 3 * WIDTH), F32),
        ((24, WIDTH), F32),
        ((24, 4 * WIDTH), F32),
        ((96, WIDTH), F32),
        ((8, 256), F32),
        ((16, 128), F32),
        ((16, 128), F32),
        ((8, 128), F32),
    )
    whole = pl.BlockSpec(memory_space=pltpu.VMEM)
    return pl.pallas_call(
        layer_kernel,
        out_shape=[jax.ShapeDtypeStruct(shape, kind) for shape, kind in shapes],
        in_specs=[pl.BlockSpec(memory_space=pl.ANY)] * len(args),
        out_specs=[whole] * len(shapes),
        scratch_shapes=[pltpu.VMEM(shape, kind) for shape, kind in SCRATCH.values()]
        + [pltpu.SMEM((3, 1), jnp.int32)]
        + [pltpu.SemaphoreType.DMA((SEM_COUNT,)), pltpu.SemaphoreType.DMA((SEM_COUNT,))],
        compiler_params=pltpu.CompilerParams(
            collective_id=0, has_side_effects=True, vmem_limit_bytes=60 * 1024 * 1024
        ),
    )(*args)


HELD = (2, 8, 9, 7, 10, 3, 4, 5, 6)


def finish_kernel(*refs):
    sources, outs, refs = refs[:28], refs[28:49], refs[49:]
    near, results, load_sems, store_sems = refs[:28], refs[28:46], refs[46], refs[47]
    norm, g_vec, own_vec, dmod, conds = near[:5]
    weights, moments = (own_vec, *near[9:14]), near[14:26]

    order = list(range(5)) + [14, 15, 9, 16, 17]
    for k in range(2, 6):
        order += [3 + k, 8 + k, 14 + 2 * k, 15 + 2 * k]
    loads = {}
    for n in order:
        source = sources[HELD[n]] if n < 9 else sources[n + 2]
        loads[n] = pltpu.make_async_copy(source, near[n], load_sems.at[n])
        loads[n].start()
    for n in (26, 27):
        loads[n] = pltpu.make_async_copy(sources[n - 26], near[n], load_sems.at[n])
        loads[n].start()
    for n in order[:10]:
        loads[n].wait()
    outs[2][0, 0] = norm[0, 0]
    clip = jnp.minimum(1.0, CLIP / (norm[0:1, 0:1] + 1e-06))
    wide, narrow = near[9].shape[0], moments[0].shape[1]
    rounded = conds[...].astype(BF).astype(F32)
    turned_mod = dmod[...].T
    g_ada = turned_mod[0:wide, 0:1] * rounded[0:1, :]
    for k in range(1, 4):
        g_ada += turned_mod[0:wide, k : k + 1] * rounded[k : k + 1, :]
    stores = []
    for k in range(6):
        if k > 1:
            for n in order[2 + 4 * k : 6 + 4 * k]:
                loads[n].wait()
        grad = g_vec[0:9, 0:narrow] if k == 0 else g_ada if k == 1 else near[3 + k][...]
        updated = adam_step(
            weights[k][...] if k else own_vec[0:9, 0:narrow],
            grad * clip,
            moments[2 * k][...],
            moments[2 * k + 1][...],
            RATE if k else RATE_VECTORS,
            DECAY if k else 0.0,
        )
        for n in range(3):
            at = 3 * k + n
            results[at][...] = updated[n]
            stores.append(pltpu.make_async_copy(results[at], outs[3 + at], store_sems.at[at]))
            stores[-1].start()
    for n in (26, 27):
        loads[n].wait()
        stores.append(pltpu.make_async_copy(near[n], outs[n - 26].at[0], store_sems.at[n - 8]))
        stores[-1].start()
    for copy in stores:
        copy.wait()


def run_finish(partial_results, weights, moments):
    shapes = [((1, ROWS, WIDTH), BF), ((1, ROWS, WIDTH), F32), ((1, 1), F32)]
    for moment in moments[::2]:
        shapes += [(moment.shape, F32)] * 3
    far = pl.BlockSpec(memory_space=pl.ANY)
    specs = [far] * len(shapes)
    specs[2] = pl.BlockSpec(memory_space=pltpu.SMEM)
    near = [partial_results[k] for k in HELD] + [*weights, *moments, *partial_results[:2]]
    args = (*partial_results, *weights, *moments)
    return pl.pallas_call(
        finish_kernel,
        out_shape=[jax.ShapeDtypeStruct(shape, kind) for shape, kind in shapes],
        in_specs=[far] * len(args),
        out_specs=specs,
        scratch_shapes=[pltpu.VMEM(array.shape, array.dtype) for array in near]
        + [pltpu.VMEM(shape, kind) for shape, kind in shapes[3:]]
        + [pltpu.SemaphoreType.DMA((28,)), pltpu.SemaphoreType.DMA((20,))],
        compiler_params=pltpu.CompilerParams(vmem_limit_bytes=60 * 1024 * 1024),
    )(*args)


def slices(
    tokens_in,
    cotangent,
    timesteps,
    span_start,
    span_len,
    vectors,
    w_ada,
    w_qkv,
    w_attn,
    w_in,
    w_out,
    m_vec,
    v_vec,
    m_ada,
    v_ada,
    m_qkv,
    v_qkv,
    m_attn,
    v_attn,
    m_in,
    v_in,
    m_out,
    v_out,
):
    partial_results = run_layer(
        timesteps,
        span_start,
        span_len,
        tokens_in,
        cotangent,
        vectors,
        w_ada.T,
        w_qkv,
        w_attn,
        w_in,
        w_out,
    )
    moments = (
        m_vec,
        v_vec,
        m_ada.T,
        v_ada.T,
        m_qkv,
        v_qkv,
        m_attn,
        v_attn,
        m_in,
        v_in,
        m_out,
        v_out,
    )
    results = run_finish(partial_results, (w_ada.T, w_qkv, w_attn, w_in, w_out), moments)
    ada_results = [result.T for result in results[6:9]]
    return (*results[:2], results[2].reshape(()), *results[3:6], *ada_results, *results[9:])


def solution(mesh):
    in_specs = (
        P("dp", "seq", None),
        P("dp", "seq", None),
        P("dp"),
        P("dp"),
        P("dp"),
        P(),
        P(None, ("dp", "seq")),
        P(("dp", "seq"), None),
        P(("dp", "seq"), None),
        P(("dp", "seq"), None),
        P(("dp", "seq"), None),
        P(None, ("dp", "seq")),
        P(None, ("dp", "seq")),
        P(None, ("dp", "seq")),
        P(None, ("dp", "seq")),
        P(("dp", "seq"), None),
        P(("dp", "seq"), None),
        P(("dp", "seq"), None),
        P(("dp", "seq"), None),
        P(("dp", "seq"), None),
        P(("dp", "seq"), None),
        P(("dp", "seq"), None),
        P(("dp", "seq"), None),
    )
    out_specs = (
        P("dp", "seq", None),
        P("dp", "seq", None),
        P(),
        P(None, ("dp", "seq")),
        P(None, ("dp", "seq")),
        P(None, ("dp", "seq")),
        P(None, ("dp", "seq")),
        P(None, ("dp", "seq")),
        P(None, ("dp", "seq")),
        P(("dp", "seq"), None),
        P(("dp", "seq"), None),
        P(("dp", "seq"), None),
        P(("dp", "seq"), None),
        P(("dp", "seq"), None),
        P(("dp", "seq"), None),
        P(("dp", "seq"), None),
        P(("dp", "seq"), None),
        P(("dp", "seq"), None),
        P(("dp", "seq"), None),
        P(("dp", "seq"), None),
        P(("dp", "seq"), None),
    )
    sizes = dict(mesh.shape)
    local = slices if (sizes["dp"], sizes["seq"]) == (4, 8) else plain
    return jax.shard_map(local, mesh=mesh, in_specs=in_specs, out_specs=out_specs, check_vma=False)
```

```python
from functools import partial
import math
from types import SimpleNamespace

import jax
import jax.numpy as jnp
from jax import lax
from jax.experimental import pallas as pl
from jax.experimental.pallas import tpu as pltpu
from jax.sharding import PartitionSpec as P

HD = 64
COND = 128
STEP = 10


BETA_ONE = 0.9
BETA_TWO = 0.999
ADAM_EPS = 1e-08
RATE = 0.1
RATE_VECTORS = 0.3
DECAY = 0.01
CLIP = 1.0
NORM_EPS = 1e-05


def cond_input(timesteps):
    half_cond = COND // 2
    freqs = jnp.exp(jnp.arange(half_cond, dtype=jnp.float32) * (-math.log(10000.0) / half_cond))
    angles = timesteps.astype(jnp.float32)[:, None] * freqs[None, :]
    return jax.nn.silu(jnp.concatenate([jnp.cos(angles), jnp.sin(angles)], axis=1))


def rotary_tables(positions):
    half_head = HD // 2
    inverse = jnp.exp(jnp.arange(half_head, dtype=jnp.float32) * (-math.log(10000.0) / half_head))
    angles = positions.astype(jnp.float32)[:, None] * inverse[None, :]
    return (jnp.cos(angles), jnp.sin(angles))


def rotate(values, cosines, sines):
    half_head = values.shape[-1] // 2
    first = values[..., :half_head]
    second = values[..., half_head:]
    cos_b = cosines[:, None, :]
    sin_b = sines[:, None, :]
    return jnp.concatenate(
        [first * cos_b - second * sin_b, second * cos_b + first * sin_b], axis=-1
    )


def rotate_back(grads, cosines, sines):
    half_head = grads.shape[-1] // 2
    first = grads[..., :half_head]
    second = grads[..., half_head:]
    cos_b = cosines[:, None, :]
    sin_b = sines[:, None, :]
    return jnp.concatenate(
        [first * cos_b + second * sin_b, second * cos_b - first * sin_b], axis=-1
    )


def normalize(values):
    centre = jnp.mean(values, axis=-1, keepdims=True)
    centred = values - centre
    inverse = lax.rsqrt(jnp.mean(centred * centred, axis=-1, keepdims=True) + NORM_EPS)
    return (centred * inverse, inverse)


def norm_back(normed, inverse, grad):
    return inverse * (
        grad
        - jnp.mean(grad, axis=-1, keepdims=True)
        - normed * jnp.mean(grad * normed, axis=-1, keepdims=True)
    )


def split_kv(block, width):
    seqs, block_rows = (block.shape[0], block.shape[1])
    keys = block[..., :width].reshape(seqs, block_rows, width // HD, HD)
    values = block[..., width:].reshape(seqs, block_rows, width // HD, HD)
    return (keys, values)


def attend_piece(carry, piece, queries, width, factor):
    piece_rows = piece.shape[1]
    size = math.gcd(piece_rows, 512)

    def attend_one_block(index, state):
        running, denom, accum = state
        block = lax.dynamic_slice_in_dim(piece, index * size, size, 1)
        keys, values = split_kv(block, width)
        scores = (
            jnp.einsum("sqhd,skhd->shqk", queries, keys, preferred_element_type=jnp.float32)
            * factor
        )
        highest = jnp.maximum(running, jnp.max(scores, axis=-1))
        shrink = jnp.exp(running - highest)
        weights = jnp.exp(scores - highest[..., None])
        denom = denom * shrink + jnp.sum(weights, axis=-1)
        accum = accum * shrink[..., None] + jnp.einsum(
            "shqk,skhd->shqd",
            weights.astype(jnp.bfloat16),
            values,
            preferred_element_type=jnp.float32,
        )
        return (highest, denom, accum)

    return lax.fori_loop(0, piece_rows // size, attend_one_block, carry)


def block_grads(block, queries, grad_out, logsum, delta, width, factor):
    keys, values = split_kv(block, width)
    scores = (
        jnp.einsum("sqhd,skhd->shqk", queries, keys, preferred_element_type=jnp.float32) * factor
    )
    probs = jnp.exp(scores - logsum[..., None])
    dprobs = jnp.einsum("sqhd,skhd->shqk", grad_out, values, preferred_element_type=jnp.float32)
    dscores = (probs * (dprobs - delta[..., None])).astype(jnp.bfloat16)
    return (keys, probs, dscores)


def query_grads(kv_all, queries, grad_out, logsum, delta, width, factor):
    total_rows = kv_all.shape[1]
    size = math.gcd(total_rows, 512)

    def query_one_block(index, accum):
        block = lax.dynamic_slice_in_dim(kv_all, index * size, size, 1)
        keys, probs, dscores = block_grads(block, queries, grad_out, logsum, delta, width, factor)
        return accum + factor * jnp.einsum(
            "shqk,skhd->sqhd", dscores, keys, preferred_element_type=jnp.float32
        )

    return lax.fori_loop(
        0, total_rows // size, query_one_block, jnp.zeros(queries.shape, jnp.float32)
    )


def key_grads(kv_all, queries, grad_out, logsum, delta, width, factor, count):
    size = math.gcd(count, 512)
    seqs = queries.shape[0]

    def key_one_block(index, accum):
        block = lax.dynamic_slice_in_dim(kv_all, index * size, size, 1)
        keys, probs, dscores = block_grads(block, queries, grad_out, logsum, delta, width, factor)
        grad_vals = jnp.einsum(
            "shqk,sqhd->skhd",
            probs.astype(jnp.bfloat16),
            grad_out,
            preferred_element_type=jnp.float32,
        )
        grad_keys = factor * jnp.einsum(
            "shqk,sqhd->skhd", dscores, queries, preferred_element_type=jnp.float32
        )
        joined = jnp.concatenate(
            [grad_keys.reshape(seqs, size, width), grad_vals.reshape(seqs, size, width)], axis=-1
        )
        return lax.dynamic_update_slice_in_dim(
            accum, jnp.transpose(joined, (1, 0, 2)), index * size, 0
        )

    initial = jnp.zeros((count, seqs, 2 * width), jnp.float32)
    return lax.fori_loop(0, count // size, key_one_block, initial)


def adam_step(weight, grad, first, second, rate, decay_rate):
    new_first = BETA_ONE * first + (1.0 - BETA_ONE) * grad
    new_second = BETA_TWO * second + (1.0 - BETA_TWO) * grad * grad
    fixed_first = new_first / (1.0 - BETA_ONE**STEP)
    fixed_second = new_second / (1.0 - BETA_TWO**STEP)
    new_weight = weight - rate * (
        fixed_first / (jnp.sqrt(fixed_second) + ADAM_EPS) + decay_rate * weight
    )
    return (new_first, new_second, new_weight)


def mod_back(grad_hidden, ln_values, normed, scale_part, gain):
    grad_shift = jnp.sum(grad_hidden, axis=1)
    grad_scale = jnp.sum(grad_hidden * ln_values, axis=1)
    grad_ln = grad_hidden * (1.0 + scale_part)
    grad_gain = jnp.sum(grad_ln * normed, axis=(0, 1))
    return (grad_shift, grad_scale, grad_gain, grad_ln * gain)


def plain(
    tokens_in,
    cotangent,
    timesteps,
    span_start,
    span_len,
    vectors,
    w_ada,
    w_qkv,
    w_attn,
    w_in,
    w_out,
    m_vec,
    v_vec,
    m_ada,
    v_ada,
    m_qkv,
    v_qkv,
    m_attn,
    v_attn,
    m_in,
    v_in,
    m_out,
    v_out,
):
    seqs, group, width = tokens_in.shape
    heads = width // HD
    factor = HD ** (-0.5)
    flat_rows = seqs * group
    full_ada, full_qkv, full_attn, full_in, full_out = (
        lax.all_gather(w_ada.astype(jnp.bfloat16), ("dp", "seq"), axis=1, tiled=True),
        lax.all_gather(w_qkv.astype(jnp.bfloat16), ("dp", "seq"), axis=0, tiled=True),
        lax.all_gather(w_attn.astype(jnp.bfloat16), ("dp", "seq"), axis=0, tiled=True),
        lax.all_gather(w_in.astype(jnp.bfloat16), ("dp", "seq"), axis=0, tiled=True),
        lax.all_gather(w_out.astype(jnp.bfloat16), ("dp", "seq"), axis=0, tiled=True),
    )
    positions = lax.axis_index("seq") * group + jnp.arange(group, dtype=jnp.int32)
    masked = (positions[None, :] >= span_start[:, None]) & (
        positions[None, :] < (span_start + span_len)[:, None]
    )
    cond_bf = cond_input(timesteps).astype(jnp.bfloat16)
    modulation = jnp.dot(cond_bf, full_ada, preferred_element_type=jnp.float32) + vectors[
        2:8
    ].reshape(1, 6 * width)
    pieces = [modulation[:, which * width : (which + 1) * width][:, None, :] for which in range(6)]
    shift_one, scale_one, gate_one, shift_two, scale_two, gate_two = pieces
    start_tokens = jnp.where(
        masked[..., None], vectors[8][None, None, :], tokens_in.astype(jnp.float32)
    )
    normed_one, inv_one = normalize(start_tokens)
    ln_one = normed_one * vectors[0]
    hidden_one = (
        (ln_one * (1.0 + scale_one) + shift_one).astype(jnp.bfloat16).reshape(flat_rows, width)
    )
    projected = jnp.dot(hidden_one, full_qkv, preferred_element_type=jnp.float32).reshape(
        seqs, group, 3 * width
    )
    cosines, sines = rotary_tables(positions)
    queries = rotate(projected[..., :width].reshape(seqs, group, heads, HD), cosines, sines).astype(
        jnp.bfloat16
    )
    keys_here = rotate(
        projected[..., width : 2 * width].reshape(seqs, group, heads, HD), cosines, sines
    ).astype(jnp.bfloat16)
    values_here = projected[..., 2 * width :].astype(jnp.bfloat16)
    kv_local = jnp.concatenate([keys_here.reshape(seqs, group, width), values_here], axis=-1)
    initial = (
        jnp.full((seqs, heads, group), -1e30, jnp.float32),
        jnp.zeros((seqs, heads, group), jnp.float32),
        jnp.zeros((seqs, heads, group, HD), jnp.float32),
    )
    running, denom, accum = attend_piece(
        initial, lax.all_gather(kv_local, "seq", axis=1, tiled=True), queries, width, factor
    )
    attn_heads = accum / denom[..., None]
    logsum = running + jnp.log(denom)
    attn_rows = jnp.transpose(attn_heads, (0, 2, 1, 3)).reshape(flat_rows, width)
    attn_bf = attn_rows.astype(jnp.bfloat16)
    branch_one = jnp.dot(attn_bf, full_attn, preferred_element_type=jnp.float32).reshape(
        seqs, group, width
    )
    mid_tokens = start_tokens + gate_one * branch_one
    normed_two, inv_two = normalize(mid_tokens)
    ln_two = normed_two * vectors[1]
    hidden_two = (
        (ln_two * (1.0 + scale_two) + shift_two).astype(jnp.bfloat16).reshape(flat_rows, width)
    )
    pre_act = jnp.dot(hidden_two, full_in, preferred_element_type=jnp.float32)
    activ, gelu_back = jax.vjp(partial(jax.nn.gelu, approximate=True), pre_act)
    activ_bf = activ.astype(jnp.bfloat16)
    branch_two = jnp.dot(activ_bf, full_out, preferred_element_type=jnp.float32).reshape(
        seqs, group, width
    )
    block_out = (mid_tokens + gate_two * branch_two).astype(jnp.bfloat16)
    grad_y = cotangent.astype(jnp.float32)
    grad_gate_two = jnp.sum(grad_y * branch_two, axis=1)
    grad_branch_two = (grad_y * gate_two).astype(jnp.bfloat16).reshape(flat_rows, width)
    grad_w_out = jnp.dot(activ_bf.T, grad_branch_two, preferred_element_type=jnp.float32)
    grad_activ = jnp.dot(grad_branch_two, full_out.T, preferred_element_type=jnp.float32)
    grad_pre = gelu_back(grad_activ)[0].astype(jnp.bfloat16)
    grad_w_in = jnp.dot(hidden_two.T, grad_pre, preferred_element_type=jnp.float32)
    grad_hidden_two = jnp.dot(grad_pre, full_in.T, preferred_element_type=jnp.float32).reshape(
        seqs, group, width
    )
    grad_shift_two, grad_scale_two, grad_gain_two, grad_normed_two = mod_back(
        grad_hidden_two, ln_two, normed_two, scale_two, vectors[1]
    )
    grad_mid = grad_y + norm_back(normed_two, inv_two, grad_normed_two)
    grad_gate_one = jnp.sum(grad_mid * branch_one, axis=1)
    grad_branch_one = (grad_mid * gate_one).astype(jnp.bfloat16).reshape(flat_rows, width)
    grad_w_attn = jnp.dot(attn_bf.T, grad_branch_one, preferred_element_type=jnp.float32)
    grad_attn_bf = (
        jnp.dot(grad_branch_one, full_attn.T, preferred_element_type=jnp.float32)
        .astype(jnp.bfloat16)
        .reshape(seqs, group, heads, HD)
    )
    delta = jnp.einsum("sqhd,shqd->shq", grad_attn_bf.astype(jnp.float32), attn_heads)
    kv_all = lax.all_gather(kv_local, "seq", axis=1, tiled=True)
    grad_queries = query_grads(kv_all, queries, grad_attn_bf, logsum, delta, width, factor)
    grad_kv = jnp.transpose(
        lax.psum_scatter(
            key_grads(
                kv_all,
                queries,
                grad_attn_bf,
                logsum,
                delta,
                width,
                factor,
                group * lax.axis_size("seq"),
            ).astype(jnp.bfloat16),
            "seq",
            scatter_dimension=0,
            tiled=True,
        ).astype(jnp.float32),
        (1, 0, 2),
    )
    grad_keys = grad_kv[..., :width].reshape(seqs, group, heads, HD)
    grad_qkv = jnp.concatenate(
        [
            rotate_back(grad_queries, cosines, sines).reshape(seqs, group, width),
            rotate_back(grad_keys, cosines, sines).reshape(seqs, group, width),
            grad_kv[..., width:],
        ],
        axis=-1,
    )
    grad_qkv = grad_qkv.astype(jnp.bfloat16).reshape(flat_rows, 3 * width)
    grad_w_qkv = jnp.dot(hidden_one.T, grad_qkv, preferred_element_type=jnp.float32)
    grad_hidden_one = jnp.dot(grad_qkv, full_qkv.T, preferred_element_type=jnp.float32).reshape(
        seqs, group, width
    )
    grad_shift_one, grad_scale_one, grad_gain_one, grad_normed_one = mod_back(
        grad_hidden_one, ln_one, normed_one, scale_one, vectors[0]
    )
    grad_start = grad_mid + norm_back(normed_one, inv_one, grad_normed_one)
    grad_mask_row = jnp.sum(jnp.where(masked[..., None], grad_start, 0.0), axis=(0, 1))
    grad_input = jnp.where(masked[..., None], 0.0, grad_start)
    grad_mod = jnp.concatenate(
        [
            grad_shift_one,
            grad_scale_one,
            grad_gate_one,
            grad_shift_two,
            grad_scale_two,
            grad_gate_two,
        ],
        axis=1,
    )
    grad_w_ada = jnp.dot(cond_bf.astype(jnp.float32).T, grad_mod, precision=lax.Precision.HIGHEST)
    grad_vectors = jnp.concatenate(
        [
            grad_gain_one[None, :],
            grad_gain_two[None, :],
            jnp.sum(grad_mod, axis=0).reshape(6, width),
            grad_mask_row[None, :],
        ],
        axis=0,
    )
    red_ada, red_qkv, red_attn, red_in, red_out, red_vec = (
        lax.psum_scatter(grad_w_ada, ("dp", "seq"), scatter_dimension=1, tiled=True),
        lax.psum_scatter(grad_w_qkv, ("dp", "seq"), scatter_dimension=0, tiled=True),
        lax.psum_scatter(grad_w_attn, ("dp", "seq"), scatter_dimension=0, tiled=True),
        lax.psum_scatter(grad_w_in, ("dp", "seq"), scatter_dimension=0, tiled=True),
        lax.psum_scatter(grad_w_out, ("dp", "seq"), scatter_dimension=0, tiled=True),
        lax.psum_scatter(grad_vectors, ("dp", "seq"), scatter_dimension=1, tiled=True),
    )
    local_squares = jnp.float32(0.0)
    for reduced in (red_vec, red_ada, red_qkv, red_attn, red_in, red_out):
        local_squares = local_squares + jnp.sum(reduced * reduced)
    grad_norm = jnp.sqrt(lax.psum(local_squares, ("dp", "seq")))
    clip_factor = jnp.minimum(1.0, CLIP / (grad_norm + 1e-06))
    columns = red_vec.shape[1]
    own_vectors = lax.dynamic_slice_in_dim(
        vectors, lax.axis_index(("dp", "seq")) * columns, columns, 1
    )
    vec_out = adam_step(own_vectors, red_vec * clip_factor, m_vec, v_vec, RATE_VECTORS, 0.0)
    ada_out = adam_step(w_ada, red_ada * clip_factor, m_ada, v_ada, RATE, DECAY)
    qkv_out = adam_step(w_qkv, red_qkv * clip_factor, m_qkv, v_qkv, RATE, DECAY)
    attn_out = adam_step(w_attn, red_attn * clip_factor, m_attn, v_attn, RATE, DECAY)
    in_out = adam_step(w_in, red_in * clip_factor, m_in, v_in, RATE, DECAY)
    out_out = adam_step(w_out, red_out * clip_factor, m_out, v_out, RATE, DECAY)
    return (
        block_out,
        grad_input,
        grad_norm,
        vec_out[0],
        vec_out[1],
        vec_out[2],
        ada_out[0],
        ada_out[1],
        ada_out[2],
        qkv_out[0],
        qkv_out[1],
        qkv_out[2],
        attn_out[0],
        attn_out[1],
        attn_out[2],
        in_out[0],
        in_out[1],
        in_out[2],
        out_out[0],
        out_out[1],
        out_out[2],
    )


F32, BF = jnp.float32, jnp.bfloat16
MESH = pl.DeviceIdType.MESH
DP, LINE, SEQ, CHIPS, ALL = 4, 4, 8, 16, 32
ROWS, WIDTH, PACK = 128, 768, 640
HALF = WIDTH // 2
HALVES = ((0, 0), (0, 1), (0, 2), (2, 2), (1, 0), (1, 1), (1, 2), None, (2, 0), (2, 1))

def numbered(**counts):
    at = {}
    for name, count in counts.items():
        at[name] = sum(counts[other] for other in at)
    return SimpleNamespace(**at), sum(counts.values())


S, SEM_COUNT = numbered(
    load=11,
    cond=1,
    mix_qkv=1,
    mix_in=1,
    mix_attn=1,
    mod=1,
    w_qkv=1,
    w_attn=4,
    plane_in=1,
    w_in=4,
    w_out=4,
    group_qkv=4,
    group_attn=4,
    fw_qkv=1,
    fw_attn=1,
    fw_in=1,
    fw_out=1,
    tok=4,
    h2=4,
    dm=4,
    xf=4,
    o=1,
    mm=1,
    dh2=1,
    do=1,
    gp=1,
    dh1=5,
    pair_out=1,
    pair_in=1,
    pair_attn=1,
    pair_qkv=1,
    plane_attn=1,
    plane_qkv=1,
    line_out=5,
    line_in=5,
    slice_in=1,
    line_attn=1,
    line_qkv=1,
    last_in=1,
    last_attn=1,
    last_qkv=1,
    early=7,
    late=7,
    sq=1,
)

SCRATCH = dict(
    i_tok=((1, 128, 768), BF),
    i_cot=((1, 128, 768), BF),
    i_vec=((9, 768), F32),
    i_wada=((144, 128), F32),
    i_wqkv=((24, 2304), F32),
    i_wattn=((24, 768), F32),
    i_win=((24, 3072), F32),
    i_wout=((96, 768), F32),
    wide_qkv=((48, 3072), F32),
    wide_in=((48, 3072), F32),
    wide_attn=((48, 768), F32),
    s_qkv=((48, 3072), BF),
    s_in=((48, 3072), BF),
    s_attn=((48, 768), BF),
    w_qkv=((768, 768), BF),
    w_in=((4, 4, 48, 768), BF),
    w_attn=((768, 768), BF),
    w_out=((4, 2, 96, 768), BF),
    t_w_qkv=((640, 768), BF),
    t_w_attn=((768, 1024), BF),
    t_w_in=((768, 768), BF),
    t_w_out=((768, 768), BF),
    t_h1=((768, 512), BF),
    conds_all=((4, 8, 128), F32),
    mod_send=((4, 4, 128), F32),
    mod_got=((32, 4, 128), F32),
    mod_flat=((40, 128), F32),
    mod_pad=((8, 384), F32),
    turn=((2, 4, 128, 128), F32),
    dmod_flat=((4, 40, 128), F32),
    mod=((8, 768), F32),
    x0=((128, 768), F32),
    n1=((4, 128, 768), F32),
    inv1=((4, 128, 128), F32),
    x1=((128, 768), F32),
    n2=((128, 768), F32),
    inv2=((128, 128), F32),
    a=((128, 768), F32),
    dx1=((128, 768), F32),
    toks=((4, 128, 768), BF),
    h1=((4, 128, 768), BF),
    h2=((4, 128, 768), BF),
    dm=((4, 128, 768), BF),
    gb=((4, 128, 768), BF),
    du=((4, 128, 768), BF),
    xb=((2, 4, 128, 640), BF),
    pt=((3, 1024, 512), BF),
    vt=((2, 128, 1024), BF),
    kt=((2, 128, 1024), BF),
    back=((4, 128, 768), F32),
    ot=((2, 128, 512), F32),
    os=((4, 192, 128), BF),
    ob=((4, 192, 128), BF),
    o2=((4, 128, 128), BF),
    mms=((4, 128, 768), BF),
    mmr=((4, 128, 768), BF),
    dhs=((4, 128, 768), BF),
    dhr=((4, 128, 768), BF),
    das=((128, 768), BF),
    dos=((4, 192, 128), BF),
    dob=((4, 192, 128), BF),
    dst=((3, 1024, 512), BF),
    ga=((512, 640), F32),
    gps=((512, 512), BF),
    gpr=((512, 512), BF),
    dqkv=((4, 128, 768), BF),
    d1s=((4, 128, 768), BF),
    d1r=((4, 128, 768), BF),
    g_out=((4, 2, 96, 768), BF),
    g_in=((2, 4, 4, 48, 384), BF),
    g_attn=((2, 768, 384), BF),
    g_qkv=((2, 768, 384), BF),
    p_out=((4, 96, 768), BF),
    p_in=((4, 4, 48, 384), BF),
    p_attn=((768, 384), BF),
    p_qkv=((768, 384), BF),
    q_attn=((4, 192, 384), BF),
    q_qkv=((4, 192, 384), BF),
    m_attn=((192, 384), BF),
    m_qkv=((192, 384), BF),
    r_out=((4, 96, 768), BF),
    r_in=((4, 4, 48, 384), BF),
    via_in=((4, 48, 384), BF),
    via_out=((96, 768), BF),
    via_dh1=((128, 768), BF),
    m_in=((4, 48, 384), BF),
    u_in=((4, 48, 384), BF),
    r_attn=((4, 48, 384), BF),
    r_qkv=((4, 48, 384), BF),
    t_in=((4, 48, 384), F32),
    t_attn=((1, 48, 384), F32),
    t_qkv=((4, 48, 384), F32),
    f_in=((4, 2, 24, 384), F32),
    f_attn=((1, 2, 24, 384), F32),
    f_qkv=((4, 2, 24, 384), F32),
    early=((8, 768), F32),
    early_pair=((8, 768), F32),
    early_line=((4, 8, 384), F32),
    early_plane=((4, 8, 384), F32),
    early_all=((2, 4, 8, 384), F32),
    late=((4, 768), F32),
    late_pair=((4, 768), F32),
    late_line=((4, 4, 384), F32),
    late_plane=((4, 4, 384), F32),
    late_all=((2, 4, 4, 384), F32),
    sq=((32, 1, 128), F32),
)


def dot(left, right):
    return jnp.dot(left, right, preferred_element_type=F32)


def dot_nt(left, right):
    return lax.dot_general(left, right, (((1,), (1,)), ((), ())), preferred_element_type=F32)


def dot_tn(left, right):
    return lax.dot_general(left, right, (((0,), (0,)), ((), ())), preferred_element_type=F32)


def loop(count, body, start=0):
    def step(index, carry):
        body(index)
        return carry

    lax.fori_loop(start, count, step, 0)


def layer_kernel(
    i_time,
    i_start,
    i_len,
    h_tok,
    h_cot,
    h_vec,
    h_wada,
    h_wqkv,
    h_wattn,
    h_win,
    h_wout,
    o_y,
    o_dx,
    o_norm,
    o_gqkv,
    o_gattn,
    o_gin,
    o_gout,
    o_dmod,
    o_gvec,
    o_vec,
    o_conds,
    *scratch,
):
    r = SimpleNamespace(**dict(zip(SCRATCH, scratch)), when=scratch[-3])
    send_sems, recv_sems = scratch[-2:]
    i_tok, i_cot, i_vec, i_wada = r.i_tok, r.i_cot, r.i_vec, r.i_wada
    i_wqkv, i_wattn, i_win, i_wout = r.i_wqkv, r.i_wattn, r.i_win, r.i_wout
    b, s = lax.axis_index("dp"), lax.axis_index("seq")
    z, c = lax.div(s, 2), lax.rem(s, 2)
    mate = s + 1 - 2 * c
    chip = b * LINE + z
    me = b * SEQ + s
    drains = []

    def push(src, dst, at, to_b, to_s, out=None):
        pltpu.make_async_remote_copy(
            src_ref=src,
            dst_ref=dst,
            send_sem=send_sems.at[at if out is None else out],
            recv_sem=recv_sems.at[at],
            device_id=(to_b, to_s),
            device_id_type=MESH,
        ).start()

    def keep(src, dst, at):
        pltpu.make_async_copy(src, dst, recv_sems.at[at]).start()

    def got(at, like):
        pltpu.make_async_copy(like, like, recv_sems.at[at]).wait()

    def left(at, like):
        pltpu.make_async_copy(like, like, send_sems.at[at]).wait()

    def sent(at, like):
        drains.append(lambda: left(at, like))

    def by_core(body):
        for h, width in ((0, HALF), (1, PACK - HALF)):

            @pl.when(c == h)
            def _():
                body(slice(HALF * h, HALF * h + width), width)

    def sent_by_core(at, like):
        drains.append(lambda: by_core(lambda columns, width: left(at, like(width))))

    near = (b, b + 1 - 2 * lax.rem(b, 2), b + 2 - 4 * lax.div(b, 2), 3 - b)

    def toward(k):
        if k == 3:
            return 3, near[3]
        slot = 1 + c if k == 1 else 2 - c
        return slot, (1 - c) * near[k] + c * near[3 - k]

    def peers(body):
        for k in (1, 2, 3):
            body(*toward(k))

    def stack(body):
        for k in (1, 2, 3):
            body(lax.rem(z + k + 2 * c * (2 - k), LINE))

    def line_gather(block, at, near=True, rest=True):
        inner = 1 + lax.rem(z, 2)
        if near:
            push(block(z), block(z), at + z, b, 2 * inner + c, at)

        def one(to):
            relayed = ((z == 1) & (to == 3)) | ((z == 2) & (to == 0))

            @pl.when(jnp.logical_not(relayed | (to == inner)))
            def _():
                push(block(z), block(z), at + z, b, 2 * to + c, at)

        if rest:
            stack(one)

    def line_relay(block, at):
        for middle, source, to in ((2, 1, 3), (1, 2, 0)):

            @pl.when(z == middle)
            def _():
                got(at + source, block(source))
                push(block(source), block(source), at + source, b, 2 * to + c, at)

    def line_got(block, at, k):
        here = (k == z) | ((z == 2) & (k == 1)) | ((z == 1) & (k == 2))

        @pl.when(jnp.logical_not(here))
        def _():
            got(at + k, block(0))

    far = lax.div(z, 2)

    def line_order(j):
        return lax.rem(z + (2, 3 - 2 * far, 1 + 2 * far, 0)[j], LINE)

    def line_add(j, rows, dst, via, at):
        to = line_order(j)
        outer_chip = (z == 0) | (z == 3)

        def direct():
            push(rows(to), dst.at[z], at + z, b, 2 * to + c, at)

        if j == 0:

            @pl.when(outer_chip)
            def _():
                push(rows(to), via, at + 4, b, 2 * (1 + far) + c, at)

            @pl.when(jnp.logical_not(outer_chip))
            def _():
                direct()

        elif j < 3:
            direct()
        else:
            keep(rows(z), dst.at[z], at + z)

    def line_via(via, at, add):
        @pl.when((z == 1) | (z == 2))
        def _():
            got(at + 4, via)
            add()

    def line_done(dst, at):
        for k in range(4):
            missing = ((z == 1) & (k == 3)) | ((z == 2) & (k == 0))

            @pl.when(jnp.logical_not(missing))
            def _():
                got(at + k, dst.at[k])

    def line_clear(dst):
        for middle, k in ((1, 3), (2, 0)):

            @pl.when(z == middle)
            def _():
                dst[k] = jnp.zeros(dst.shape[1:], BF)

    lane = lax.broadcasted_iota(jnp.int32, (1, 128), 1)
    low = lane < 64
    own24 = pl.ds(pl.multiple_of(24 * c, 8), 24)
    mate24 = pl.ds(pl.multiple_of(24 * (1 - c), 8), 24)
    part = pl.ds(pl.multiple_of(HALF * c, 128), HALF)
    chip_rows = pl.ds(pl.multiple_of(48 * chip, 16), 48)
    group_rows = pl.ds(pl.multiple_of(192 * b, 16), 192)

    barrier = pltpu.get_barrier_semaphore()

    def greet(k):
        other = lax.rem(me + k, ALL)
        pl.semaphore_signal(
            barrier, inc=1, device_id=(lax.div(other, SEQ), lax.rem(other, SEQ)), device_id_type=MESH
        )

    loads = (
        (i_time, r.when.at[0]),
        (i_start, r.when.at[1]),
        (i_len, r.when.at[2]),
        (h_wqkv, i_wqkv),
        (h_win, i_win),
        (h_wattn, i_wattn),
        (h_wout, i_wout),
        (h_tok, i_tok),
        (h_vec, i_vec),
        (h_wada, i_wada),
        (h_cot, i_cot),
    )
    for k, (src, dst) in enumerate(loads):
        pltpu.make_async_copy(src, dst, recv_sems.at[S.load + k]).start()
    loop(ALL, greet, 1)
    for k, (src, dst) in enumerate(loads):
        pltpu.make_async_copy(src, dst, recv_sems.at[S.load + k]).wait()

    def natural(kind, p, head):
        return kind * WIDTH + 192 * p + 64 * head

    def half_at(ref, column, high):
        tile = ref[:, column // 128 * 128 : column // 128 * 128 + 128]
        return tile if (column % 128 == 64) == high else pltpu.roll(tile, 64, 1)

    for p in range(4):
        for tile in range(5):
            pair = []
            for high in (0, 1):
                which = HALVES[2 * tile + high]
                pair.append(
                    jnp.zeros((24, 128), F32)
                    if which is None
                    else half_at(i_wqkv, natural(which[0], p, which[1]), bool(high))
                )
            r.wide_qkv[own24, 768 * p + 128 * tile : 768 * p + 128 * tile + 128] = jnp.where(
                low, pair[0], pair[1]
            )
        r.wide_qkv[own24, 768 * p + 640 : 768 * p + 768] = jnp.zeros((24, 128), F32)
    r.wide_in[own24, :] = i_win[...]
    r.wide_attn[own24, :] = i_wattn[...]
    r.w_out[z, c] = i_wout[...].astype(BF)
    r.toks[z] = i_tok[0]
    line_clear(r.r_out)
    line_clear(r.r_in)
    line_clear(r.d1r)
    for ref in (r.q_qkv, r.r_qkv):
        ref[:, :, PACK - HALF : HALF] = jnp.zeros((4, ref.shape[1], WIDTH - PACK), BF)
    lanes8 = lax.broadcasted_iota(jnp.int32, (8, 128), 1)
    half_cond = COND // 2
    speed = jnp.exp((lanes8 % half_cond).astype(F32) * (-math.log(10000.0) / half_cond))
    angle = r.when[0, 0].astype(F32) * speed
    wave = jnp.where(lanes8 < half_cond, jnp.cos(angle), jnp.sin(angle))
    r.conds_all[b] = wave * (1.0 / (1.0 + jnp.exp(-wave)))
    pl.semaphore_wait(barrier, ALL - 1)

    def token_block(k):
        return r.toks.at[k]

    def attn_block(k):
        return r.w_attn.at[pl.ds(pl.multiple_of(192 * b + 48 * k, 16), 48), part]

    def in_block(k):
        return r.w_in.at[:, k, :, part]

    def out_block(k):
        return r.w_out.at[k, c]

    peers(lambda k, to: push(r.conds_all.at[b], r.conds_all.at[b], S.cond, to, s))
    sent(S.cond, r.conds_all.at[0:3])
    push(r.wide_qkv.at[own24], r.wide_qkv.at[own24], S.mix_qkv, b, mate)
    sent(S.mix_qkv, r.wide_qkv.at[0:24])
    push(r.wide_attn.at[own24], r.wide_attn.at[own24], S.mix_attn, b, mate)
    sent(S.mix_attn, r.wide_attn.at[0:24])
    push(r.wide_in.at[own24], r.wide_in.at[own24], S.mix_in, b, mate)
    sent(S.mix_in, r.wide_in.at[0:24])

    got(S.cond, r.conds_all.at[0:3])
    row8 = lax.broadcasted_iota(jnp.int32, (8, 128), 0)
    cond4 = jnp.zeros((8, 128), F32)
    for k in range(4):
        cond4 = jnp.where(row8 == k, r.conds_all[k], cond4)
    o_conds[...] = cond4
    wide = i_wada.shape[0]
    r.mod_pad[...] = jnp.zeros((8, 384), F32)
    r.mod_pad[:, 0:wide] = dot_nt(cond4.astype(BF), i_wada[...].astype(BF))
    columns = pltpu.roll(r.mod_pad[...], lax.rem(wide * me, 128), 1)
    for k in range(4):
        for t in range(3):
            r.mod_send[k, t : t + 1, :] = columns[k : k + 1, 128 * t : 128 * t + 128]
        r.mod_send[k, 3:4, :] = jnp.zeros((1, 128), F32)

    def send_mod(k):
        other = lax.rem(me + k, ALL)
        ob = lax.div(other, SEQ)
        push(r.mod_send.at[ob], r.mod_got.at[me], S.mod, ob, lax.rem(other, SEQ))

    loop(ALL, send_mod, 1)
    sent(S.mod, r.mod_got.at[0:31])
    keep(r.mod_send.at[b], r.mod_got.at[me], S.mod)

    def block(src, first):
        return src.at[:, pl.ds(pl.multiple_of(first, 128), HALF)]

    def slices_along_line():
        def send(columns, width):
            def rows(to):
                first = pl.multiple_of(WIDTH * to + columns.start, 128)
                return r.s_qkv.at[:, pl.ds(first, width)]

            dst = r.w_qkv.at[chip_rows, columns]
            stack(lambda to: push(rows(to), dst, S.w_qkv, b, 2 * to + c))
            keep(rows(z), dst, S.w_qkv)

        by_core(send)
        sent_by_core(S.w_qkv, lambda width: r.w_qkv.at[0:144, 0:width])

    def over_plane(dst, at):
        rows = dst.at[group_rows, part]
        peers(lambda k, to: push(rows, rows, at + k, to, s))
        for k in (1, 2, 3):
            sent(at + k, dst.at[0:192, 0:HALF])

    def share(dst, at, onward):
        for k in range(4):
            rows = dst.at[pl.ds(pl.multiple_of(192 * near[k], 16), 192), part]
            if k:
                got(at + k, rows)
            push(rows, rows, onward, b, mate)
        sent(onward, dst.at[:, 0:HALF])

    def line_share(block, at, onward):
        for k in range(4):
            line_got(block, at, k)
            push(block(k), block(k), onward, b, mate)

    got(S.mix_qkv, r.wide_qkv.at[0:24])
    r.s_qkv[...] = r.wide_qkv[...].astype(BF)
    slices_along_line()
    line_gather(token_block, S.tok, rest=False)
    sent(S.tok, r.toks.at[0:3])
    got(S.mix_attn, r.wide_attn.at[0:24])
    r.s_attn[...] = r.wide_attn[...].astype(BF)

    def qkv_over_plane(columns, width):
        got(S.w_qkv, r.w_qkv.at[0:192, 0:width])
        rows = r.w_qkv.at[group_rows, columns]
        peers(lambda k, to: push(rows, rows, S.group_qkv + k, to, s))

    by_core(qkv_over_plane)
    for k in (1, 2, 3):
        sent_by_core(S.group_qkv + k, lambda width: r.w_qkv.at[0:192, 0:width])
    line_gather(token_block, S.tok, near=False)
    for h in range(2):

        @pl.when(c == h)
        def _():
            r.w_attn[chip_rows, 384 * h : 384 * h + 384] = r.s_attn[:, 384 * h : 384 * h + 384]

    line_gather(attn_block, S.w_attn)
    sent(S.w_attn, r.w_attn.at[0:144, 0:HALF])
    line_gather(out_block, S.w_out)
    sent(S.w_out, r.w_out.at[0:3, 0])
    got(S.mix_in, r.wide_in.at[0:24])
    r.s_in[...] = r.wide_in[...].astype(BF)
    peers(
        lambda k, to: push(
            block(r.s_in, WIDTH * to + HALF * c), r.w_in.at[b, z, :, part], S.plane_in, to, s
        )
    )
    keep(block(r.s_in, WIDTH * b + HALF * c), r.w_in.at[b, z, :, part], S.plane_in)
    sent(S.plane_in, r.w_in.at[0:3, 0, :, 0:HALF])

    def hidden_rows(k):
        place = (2 * k + c) * ROWS + lax.broadcasted_iota(jnp.int32, (ROWS, 1), 0)
        return (place >= r.when[1, 0]) & (place < r.when[1, 0] + r.when[2, 0])

    def first_norm(tokens, k):
        x0 = jnp.where(hidden_rows(k), i_vec[8:9, :], tokens.astype(F32))
        normed, inverse = normalize(x0)
        r.n1[k] = normed
        r.inv1[k] = jnp.broadcast_to(inverse, (ROWS, 128))
        return x0

    r.x0[...] = first_norm(i_tok[0], z)

    got(S.mod, r.mod_got)
    r.mod_flat[...] = jnp.zeros((40, 128), F32)
    for k in range(ALL):
        first = 9 * k // 8
        r.mod_flat[first : first + 3, :] += r.mod_got[k, 0:3, :]
    for k in range(6):
        row = jnp.concatenate(
            [r.mod_flat[6 * k + t : 6 * k + t + 1, :] for t in range(6)], axis=1
        )
        r.mod[k : k + 1, :] = row + i_vec[2 + k : 3 + k, :]

    def mod(k):
        return r.mod[k : k + 1, :]

    def vec(k):
        return i_vec[k : k + 1, :]

    r.h1[z] = (r.n1[z] * vec(0) * (1.0 + mod(1)) + mod(0)).astype(BF)
    r.dm[0] = (i_cot[0].astype(F32) * mod(5)).astype(BF)
    peers(lambda k, to: push(r.dm.at[0], r.dm.at[k], S.dm + k, to, s))
    for k in (1, 2, 3):
        sent(S.dm + k, r.dm.at[0])


    line_relay(token_block, S.tok)

    lanes = lax.broadcasted_iota(jnp.int32, (ROWS, 128), 1)
    first_half = lanes % HD < HD // 2
    speed = jnp.exp((lanes % (HD // 2)).astype(F32) * (-math.log(10000.0) / (HD // 2)))
    row = lax.broadcasted_iota(jnp.int32, (ROWS, 128), 0)

    def table(k):
        angle = ((2 * k + c) * ROWS + row).astype(F32) * speed
        r.turn[0, k] = jnp.cos(angle)
        sine = jnp.sin(angle)
        r.turn[1, k] = jnp.where(first_half, -sine, sine)

    loop(LINE, table)

    def qkv_share(columns, width):
        for k in range(4):
            rows = r.w_qkv.at[pl.ds(pl.multiple_of(192 * near[k], 16), 192), columns]
            if k:
                got(S.group_qkv + k, rows)
            push(rows, rows, S.fw_qkv, b, mate)

    by_core(qkv_share)
    sent_by_core(S.fw_qkv, lambda width: r.w_qkv.at[:, 0:width])
    by_core(lambda columns, width: got(S.fw_qkv, r.w_qkv.at[:, 0 : PACK - width]))
    for k in range(5):
        columns = slice(128 * k, 128 * k + 128)
        r.t_w_qkv[columns, :] = r.w_qkv[:, columns].T

    def turned(tile, sign, k):
        other = jnp.where(first_half, pltpu.roll(tile, 96, 1), pltpu.roll(tile, 32, 1))
        return tile * r.turn[0, k] + sign * (other * r.turn[1, k])

    def project(j):
        k = lax.rem(z + j, LINE)

        @pl.when(j > 0)
        def _():
            line_got(token_block, S.tok, k)
            first_norm(r.toks[k], k)
            r.h1[k] = (r.n1[k] * vec(0) * (1.0 + mod(1)) + mod(0)).astype(BF)

        x = dot(r.h1[k], r.w_qkv[:, 0:PACK])
        tiles = [x[:, 128 * t : 128 * t + 128] for t in range(5)]
        tiles[0] = turned(tiles[0], 1.0, k) * 0.125
        tiles[1] = jnp.where(low, turned(tiles[1], 1.0, k) * 0.125, tiles[1])
        tiles[2] = turned(tiles[2], 1.0, k)
        tiles[3] = turned(tiles[3], 1.0, k)
        for t in range(5):
            r.xb[0, k, :, 128 * t : 128 * t + 128] = tiles[t].astype(BF)
        push(r.xb.at[0, k], r.xb.at[1, k], S.xf + k, b, mate)

    loop(4, project)
    for k in range(4):
        sent(S.xf + k, r.xb.at[0, 0])

    for k in range(6):
        columns = slice(128 * k, 128 * k + 128)
        r.t_h1[columns, :] = r.h1[:, :, columns].reshape(512, 128).T
    for k in range(4):
        got(S.xf + k, r.xb.at[0, 0])

    def tile_of(t):
        return r.xb[:, :, :, 128 * t : 128 * t + 128].reshape(1024, 128)

    heads = ((0, 2, 4, True, True), (0, 2, 4, False, False), (1, 3, 1, True, False))

    def queries(head, first, size):
        q_tile, _, _, q_low, _ = heads[head]
        q = r.xb[0, first : first + size, :, 128 * q_tile : 128 * q_tile + 128]
        return jnp.where(low if q_low else ~low, q.reshape(size * 128, 128), jnp.zeros((), BF))

    r.vt[0] = tile_of(4).T
    r.vt[1] = tile_of(1).T
    for half in range(2):
        at = slice(256 * half, 256 * half + 256)
        for head in range(3):
            scores = dot_nt(tile_of(heads[head][1]), queries(head, 2 * half, 2))
            weights = jnp.exp(scores - jnp.max(scores, axis=0, keepdims=True))
            weights = weights * (1.0 / jnp.sum(weights, axis=0, keepdims=True))
            weights = weights.astype(BF)
            r.pt[head, :, at] = weights
            out = dot(r.vt[head // 2], weights)
            if head == 0:
                r.ot[0, 0:64, at] = out[0:64]
            elif head == 1:
                r.ot[0, 64:128, at] = out[64:128]
            else:
                r.ot[1, 0:64, at] = out[64:128]
                r.ot[1, 64:128, at] = jnp.zeros((64, 256), F32)
        for k in (2 * half, 2 * half + 1):
            across = slice(128 * k, 128 * k + 128)
            r.os[k, 0:128, :] = r.ot[0, :, across].T.astype(BF)
            third = r.ot[1, 0:64, across]
            third = jnp.concatenate([third, pltpu.roll(third, 64, 1)], axis=0)
            r.os[k, 128:192, :] = third.T[0:64].astype(BF)
        for to in (2 * half, 2 * half + 1):

            @pl.when(z == to)
            def _():
                keep(r.os.at[to], r.ob.at[z], S.o)

            @pl.when(z != to)
            def _():
                push(r.os.at[to], r.ob.at[z], S.o, b, 2 * to + c)

        if half == 0:
            line_relay(attn_block, S.w_attn)
            for k in range(4):
                line_got(attn_block, S.w_attn, k)
            over_plane(r.w_attn, S.group_attn)

    sent(S.o, r.os.at[0:3])
    line_relay(out_block, S.w_out)
    got(S.plane_in, r.w_in.at[:, 0, :, 0:HALF])
    line_gather(in_block, S.w_in)
    sent(S.w_in, r.w_in.at[0:3, :, :, 0:HALF])
    for k in range(2):
        r.kt[k] = tile_of(2 + k).T
    share(r.w_attn, S.group_attn, S.fw_attn)
    got(S.fw_attn, r.w_attn.at[:, 0:HALF])
    for p in range(4):
        first = 192 * p
        r.t_w_attn[:, 256 * p : 256 * p + 128] = r.w_attn[first : first + 128, :].T
        third = r.w_attn[first + 128 : first + 192, :]
        r.t_w_attn[:, 256 * p + 128 : 256 * p + 256] = jnp.concatenate(
            [third, jnp.zeros_like(third)], axis=0
        ).T
    got(S.o, r.ob)
    a = jnp.zeros((ROWS, WIDTH), F32)
    for p in range(4):
        third = r.ob[p, 128:192, :].astype(F32)
        third = jnp.concatenate([third, pltpu.roll(third, 64, 1)], axis=0)
        r.o2[p] = jnp.where(low, third, 0.0).astype(BF)
        a += dot(r.ob[p, 0:128, :], r.w_attn[192 * p : 192 * p + 128, :])
        a += dot(r.o2[p, :, 0:64], r.w_attn[192 * p + 128 : 192 * p + 192, :])
    r.a[...] = a
    x1 = r.x0[...] + mod(2) * a
    r.x1[...] = x1
    n2, inv2 = normalize(x1)
    r.n2[...] = n2
    r.inv2[...] = jnp.broadcast_to(inv2, (ROWS, 128))
    r.h2[0] = (n2 * vec(1) * (1.0 + mod(4)) + mod(3)).astype(BF)
    peers(lambda k, to: push(r.h2.at[0], r.h2.at[k], S.h2 + k, to, s))
    for k in (1, 2, 3):
        sent(S.h2 + k, r.h2.at[0])
    line_relay(in_block, S.w_in)
    line_share(out_block, S.w_out, S.fw_out)
    sent(S.fw_out, r.w_out.at[:, 0])
    got(S.fw_out, r.w_out.at[:, 0])

    for k in range(6):
        columns = slice(128 * k, 128 * k + 128)
        r.t_w_out[columns, :] = r.w_out[:, :, :, columns].reshape(WIDTH, 128).T

    def feed_back(k):
        @pl.when(k > 0)
        def _():
            got(S.dm + k, r.dm.at[0])

        r.back[k] = dot(r.dm[k], r.t_w_out[...])

    loop(4, feed_back)
    line_share(in_block, S.w_in, S.fw_in)
    sent(S.fw_in, r.w_in.at[:, :, :, 0:HALF])
    got(S.fw_in, r.w_in.at[:, :, :, 0:HALF])
    for k in range(6):
        columns = slice(128 * k, 128 * k + 128)
        r.t_w_in[columns, :] = r.w_in[:, :, :, columns].reshape(WIDTH, 128).T

    def feed(first, count):
        at = slice(first, first + count)
        size = count * ROWS
        u = dot(r.h2[at].reshape(size, WIDTH), r.w_in[...].reshape(WIDTH, WIDTH))
        slope = 0.7978845608028654
        cube = 0.044715
        t = jnp.tanh(slope * (u + cube * u * u * u))
        r.gb[at] = (0.5 * u * (1.0 + t)).astype(BF).reshape(count, ROWS, WIDTH)
        bend = 0.5 * (1.0 + t) + 0.5 * u * (1.0 - t * t) * (slope * (1.0 + 3.0 * cube * u * u))
        du = (r.back[at].reshape(size, WIDTH) * bend).astype(BF)
        r.du[at] = du.reshape(count, ROWS, WIDTH)
        r.dhs[at] = dot(du, r.t_w_in[...]).astype(BF).reshape(count, ROWS, WIDTH)

    feed(0, 1)
    for first, count in ((1, 2), (3, 1)):
        for k in range(first, first + count):
            got(S.h2 + k, r.h2.at[0])
        feed(first, count)
        for k in range(first, first + count):
            slot, to = toward(k)
            push(r.dhs.at[slot], r.dhr.at[slot], S.dh2, to, s)
    sent(S.dh2, r.dhs.at[0:3])
    def gather(own, others):
        total = own[0].astype(F32)
        for k in (1, 2, 3):
            total += others[k].astype(F32)
        return total

    for k in range(2):
        rows = slice(384 * k, 384 * k + 384)
        result = dot_tn(r.gb[:, :, rows].reshape(512, 384), r.dm[...].reshape(512, 768))
        r.g_out[2 * k : 2 * k + 2] = result.astype(BF).reshape(2, 2, 96, 768)
    push(r.g_out.at[:, 1 - c], r.p_out, S.pair_out, b, mate)
    sent(S.pair_out, r.p_out)

    def to_mate(grad, dst, at):
        push(grad.at[1 - c], dst, at, b, mate)
        sent(at, dst)

    def pair_sum(grad, pair, at):
        got(at, pair)
        grad[c] = (grad[c].astype(F32) + pair[...].astype(F32)).astype(BF)

    def plane_sum(grad, dst, at, packed=False):
        def send(columns, width):
            def rows(to):
                return grad.at[c, pl.ds(pl.multiple_of(192 * to, 16), 192), 0:width]

            peers(lambda k, to: push(rows(to), dst.at[k, :, 0:width], at, to, s))
            keep(rows(b), dst.at[0, :, 0:width], at)

        if packed:
            by_core(send)
            sent_by_core(at, lambda width: dst.at[0:3, :, 0:width])
        else:
            send(None, HALF)
            sent(at, dst.at[0:3])

    def line_sum(src, total, dst, first, at, packed=False):
        def send(columns, width):
            got(first, src.at[:, :, 0:width])
            total[...] = (
                (src[0].astype(F32) + src[1].astype(F32))
                + (src[2].astype(F32) + src[3].astype(F32))
            ).astype(BF)

            def rows(to):
                return total.at[pl.ds(pl.multiple_of(48 * to, 16), 48), 0:width]

            stack(lambda to: push(rows(to), dst.at[z, :, 0:width], at, b, 2 * to + c))
            keep(rows(z), dst.at[z, :, 0:width], at)

        if packed:
            by_core(send)
            sent_by_core(at, lambda width: dst.at[0:3, :, 0:width])
        else:
            send(None, HALF)
            sent(at, dst.at[0:3])

    def trade(total, final, at):
        push(total.at[:, mate24], final.at[:, c], at, b, mate)
        sent(at, final.at[:, 0])
        final[:, c] = total[:, own24, :]

    def in_product(k):
        rows = slice(384 * k, 384 * k + 384)
        result = dot_tn(r.h2[:, :, rows].reshape(512, 384), r.du[...].reshape(512, 768)).astype(BF)
        for h in range(2):
            r.g_in[h, 2 * k : 2 * k + 2] = result[:, 384 * h : 384 * h + 384].reshape(2, 4, 48, 384)

    in_product(0)

    got(S.pair_out, r.p_out)
    for k in range(4):
        r.g_out[k, c] = (r.g_out[k, c].astype(F32) + r.p_out[k].astype(F32)).astype(BF)

    def out_rows(k):
        return r.g_out.at[k, c]

    for j in (0, 1):
        line_add(j, out_rows, r.r_out, r.via_out, S.line_out)
    in_product(1)
    to_mate(r.g_in, r.p_in, S.pair_in)

    def add_out():
        k = line_order(2)
        r.g_out[k, c] = (r.g_out[k, c].astype(F32) + r.via_out[...].astype(F32)).astype(BF)

    got(S.dh2, r.dhr.at[0:3])
    dh = gather(r.dhs, r.dhr)
    n2 = r.n2[...]
    inv2 = r.inv2[:, 0:1]
    r.early[...] = jnp.zeros((8, 768), F32)
    r.early[2:3, :] = jnp.sum(dh, axis=0, keepdims=True)
    both = jnp.sum(dh * n2, axis=0, keepdims=True)
    r.early[3:4, :] = both * vec(1)
    r.early[0:1, :] = both * (1.0 + mod(4))
    grad = dh * ((1.0 + mod(4)) * vec(1))
    dx1 = i_cot[0].astype(F32) + norm_back(n2, inv2, grad)
    r.dx1[...] = dx1
    r.early[1:2, :] = jnp.sum(dx1 * r.a[...], axis=0, keepdims=True)
    r.das[...] = (dx1 * mod(2)).astype(BF)
    for p in range(4):
        result = dot(r.das[...], r.t_w_attn[:, 256 * p : 256 * p + 256])
        r.dos[p, 0:128, :] = result[:, 0:128].astype(BF)
        third = result[:, 128:256]
        third = jnp.where(low, third[0:64], pltpu.roll(third[64:128], 64, 1))
        r.dos[p, 128:192, :] = third.astype(BF)
    stack(lambda to: push(r.dos.at[to], r.dob.at[z], S.do, b, 2 * to + c))
    keep(r.dos.at[z], r.dob.at[z], S.do)
    sent(S.do, r.dos.at[0:3])
    for t in range(3):
        at = slice(256 * t, 256 * t + 256)
        mm = dot(r.gb[...].reshape(512, WIDTH), r.w_out[:, :, :, at].reshape(WIDTH, 256))
        r.mms[:, :, at] = mm.astype(BF).reshape(4, ROWS, 256)
    peers(lambda k, to: push(r.mms.at[k], r.mmr.at[k], S.mm, to, s))
    sent(S.mm, r.mms.at[0:3])

    for p in range(4):
        for rows, left_side in (
            (slice(192 * p, 192 * p + 128), r.ob[p, 0:128, :]),
            (slice(192 * p + 128, 192 * p + 192), r.o2[p]),
        ):
            result = dot_tn(left_side, r.das[...])[0 : rows.stop - rows.start].astype(BF)
            r.g_attn[0, rows, :] = result[:, 0:HALF]
            r.g_attn[1, rows, :] = result[:, HALF:WIDTH]
    to_mate(r.g_attn, r.p_attn, S.pair_attn)

    def small_sum(src, pair, line, plane, whole, at):
        def first():
            push(src, pair, at, b, mate)
            sent(at, src)

        def second():
            got(at, pair)
            total = src[...] + pair[...]
            line[z] = (1 - c) * total[:, 0:HALF] + c * total[:, HALF:WIDTH]
            stack(lambda to: push(line.at[z], line.at[z], at + 1, b, 2 * to + c))
            sent(at + 1, line.at[0:3])

        def third():
            got(at + 1, line.at[0:3])
            plane[b] = (line[0] + line[1]) + (line[2] + line[3])
            peers(lambda k, to: push(plane.at[b], plane.at[b], at + 2, to, s))
            sent(at + 2, plane.at[0:3])

        def fourth():
            got(at + 2, plane.at[0:3])
            whole[c] = plane[...]
            push(plane, whole.at[c], at + 3, b, mate)
            sent(at + 3, plane)

        def rows(k):
            return jnp.concatenate([whole[0, k], whole[1, k]], axis=1)

        return first, second, third, fourth, rows

    early_steps = small_sum(
        r.early, r.early_pair, r.early_line, r.early_plane, r.early_all, S.early
    )
    late_steps = small_sum(r.late, r.late_pair, r.late_line, r.late_plane, r.late_all, S.late)

    pair_sum(r.g_in, r.p_in, S.pair_in)
    line_via(r.via_out, S.line_out, add_out)
    for j in (2, 3):
        line_add(j, out_rows, r.r_out, r.via_out, S.line_out)
    sent(S.line_out, r.r_out.at[0:3])

    def in_rows(k):
        return r.g_in.at[c, :, k]

    for j in (0, 1):
        line_add(j, in_rows, r.r_in, r.via_in, S.line_in)

    def add_in():
        k = line_order(2)
        r.g_in[c, :, k] = (r.g_in[c, :, k].astype(F32) + r.via_in[...].astype(F32)).astype(BF)

    pair_sum(r.g_attn, r.p_attn, S.pair_attn)
    plane_sum(r.g_attn, r.q_attn, S.plane_attn)

    got(S.do, r.dob)
    dot0 = r.dob[:, 0:128, :].reshape(512, 128)
    third = r.dob[:, 128:192, :].astype(F32).reshape(256, 128)
    other_rows = jnp.where(low, pltpu.roll(third, 64, 1), 0.0).reshape(4, 64, 128)
    third = jnp.where(low, third, 0.0).reshape(4, 64, 128)
    dot1 = jnp.concatenate([third, other_rows], axis=1).reshape(512, 128)
    zero = jnp.zeros((), BF)
    moved = pltpu.roll(dot1, 64, 1).astype(BF)
    grads = (jnp.where(low, dot0, zero), jnp.where(low, zero, dot0), moved)
    product = dot0.astype(F32).T * r.ot[0]
    deltas = (
        jnp.sum(product[0:64], axis=0, keepdims=True),
        jnp.sum(product[64:128], axis=0, keepdims=True),
        jnp.sum(dot1.T * r.ot[1], axis=0, keepdims=True),
    )
    for head in range(3):
        values = tile_of(heads[head][2])
        for half in range(2):
            at = slice(256 * half, 256 * half + 256)
            dp = dot_nt(values, grads[head][at])
            r.dst[head, :, at] = (
                r.pt[head, :, at].astype(F32) * (dp - deltas[head][:, at])
            ).astype(BF)

    def key_grads(rows):
        dk = [dot(r.dst[head, rows, :], queries(head, 0, 4)) for head in range(3)]
        dv = [dot(r.pt[head, rows, :], grads[head]) for head in range(3)]
        return (dv[2], dk[0] + dk[1], dk[2], dv[0] + dv[1])

    line_via(r.via_in, S.line_in, add_in)
    for j in (2, 3):
        line_add(j, in_rows, r.r_in, r.via_in, S.line_in)
    sent(S.line_in, r.r_in.at[0:3])
    for t, tile in enumerate(key_grads(slice(512, 1024))):
        r.gps[:, 128 * t : 128 * t + 128] = tile.astype(BF)
    push(r.gps, r.gpr, S.gp, b, mate)
    sent(S.gp, r.gps)
    for t, tile in enumerate(key_grads(slice(0, 512))):
        r.ga[:, 128 * t + 128 : 128 * t + 256] = tile
    for half in range(2):
        at = slice(256 * half, 256 * half + 256)
        turned_q = [dot(r.kt[head // 2], r.dst[head, :, at]) for head in range(3)]
        top = jnp.concatenate([turned_q[0][0:64], turned_q[1][64:128]], axis=0)
        r.ga[at, 0:128] = top.T * 0.125
        r.ga[at, 128:256] += turned_q[2].T * 0.125
    got(S.gp, r.gpr)

    def dh1_rows(k):
        return r.d1s.at[k]

    def back_turn(k):
        rows = pl.ds(pl.multiple_of(128 * k, 128), 128)
        tiles = [r.ga[rows, 0:128]] + [
            r.ga[rows, 128 * t : 128 * t + 128]
            + r.gpr[rows, 128 * t - 128 : 128 * t].astype(F32)
            for t in range(1, 5)
        ]
        tiles[0] = turned(tiles[0], -1.0, k)
        tiles[1] = jnp.where(low, turned(tiles[1], -1.0, k), tiles[1])
        tiles[2] = turned(tiles[2], -1.0, k)
        tiles[3] = turned(tiles[3], -1.0, k)
        for t in range(5):
            r.dqkv[k, :, 128 * t : 128 * t + 128] = tiles[t].astype(BF)
        r.dqkv[k, :, PACK:WIDTH] = jnp.zeros((128, 128), BF)

    back_turn(line_order(0))

    def unproject(j):
        k = line_order(j)
        partial_sum = dot(r.dqkv[k, :, 0:PACK], r.t_w_qkv[...])
        r.d1s[k] = partial_sum.astype(BF)
        if j == 2:

            def add():
                r.d1s[k] = (partial_sum + r.via_dh1[...].astype(F32)).astype(BF)

            line_via(r.via_dh1, S.dh1, add)
        line_add(j, dh1_rows, r.d1r, r.via_dh1, S.dh1)
        n = r.n1[k]
        e = partial_sum * ((1.0 + mod(1)) * vec(0))
        weight = jnp.where(hidden_rows(k), r.inv1[k][:, 0:1], 0.0)
        centred = (
            e
            - jnp.mean(e, axis=-1, keepdims=True)
            - n * jnp.mean(e * n, axis=-1, keepdims=True)
        )
        r.late[0:1, :] += jnp.sum(partial_sum * n, axis=0, keepdims=True)
        r.late[1:2, :] += jnp.sum(partial_sum, axis=0, keepdims=True)
        r.late[3:4, :] += jnp.sum(weight * centred, axis=0, keepdims=True)

    r.late[...] = jnp.zeros((4, 768), F32)
    r.late[3:4, :] = jnp.sum(
        jnp.where(hidden_rows(z), r.dx1[...], 0.0), axis=0, keepdims=True
    )
    unproject(0)
    for j in (1, 2, 3):
        back_turn(line_order(j))

    def qkv_rows(k):
        rows = pl.ds(pl.multiple_of(128 * k, 128), 128)
        result = dot(r.t_h1[rows, :], r.dqkv[...].reshape(512, WIDTH)).astype(BF)
        r.g_qkv[0, rows, :] = result[:, 0:HALF]
        r.g_qkv[1, rows, :] = result[:, HALF:WIDTH]

    loop(6, qkv_rows)
    to_mate(r.g_qkv, r.p_qkv, S.pair_qkv)
    unproject(1)
    pair_sum(r.g_qkv, r.p_qkv, S.pair_qkv)
    plane_sum(r.g_qkv, r.q_qkv, S.plane_qkv, True)
    got(S.mm, r.mmr.at[0:3])
    mm = gather(r.mms, r.mmr)
    o_y[...] = (r.x1[...] + mod(5) * mm).astype(BF)
    r.early[4:5, :] = jnp.sum(i_cot[0].astype(F32) * mm, axis=0, keepdims=True)
    early_steps[0]()
    unproject(2)
    unproject(3)
    sent(S.dh1, r.d1s.at[0:3])
    both = r.late[0:1, :]
    r.late[2:3, :] = both * vec(0)
    r.late[0:1, :] = both * (1.0 + mod(1))
    late_steps[0]()
    early_steps[1]()
    line_sum(r.q_attn, r.m_attn, r.r_attn, S.plane_attn, S.line_attn)
    late_steps[1]()

    line_done(r.r_in, S.line_in)
    r.m_in[...] = (
        (r.r_in[0].astype(F32) + r.r_in[1].astype(F32))
        + (r.r_in[2].astype(F32) + r.r_in[3].astype(F32))
    ).astype(BF)
    peers(lambda k, to: push(r.m_in.at[to], r.u_in.at[b], S.slice_in, to, s))
    keep(r.m_in.at[b], r.u_in.at[b], S.slice_in)
    sent(S.slice_in, r.u_in.at[0:3])
    line_sum(r.q_qkv, r.m_qkv, r.r_qkv, S.plane_qkv, S.line_qkv, True)
    early_steps[2]()
    late_steps[2]()

    line_done(r.d1r, S.dh1)
    dh = (r.d1r[0].astype(F32) + r.d1r[1].astype(F32)) + (
        r.d1r[2].astype(F32) + r.d1r[3].astype(F32)
    )
    n1 = r.n1[z]
    grad = dh * ((1.0 + mod(1)) * vec(0))
    dx0 = r.dx1[...] + norm_back(n1, r.inv1[z][:, 0:1], grad)
    o_dx[...] = jnp.where(hidden_rows(z), 0.0, dx0)
    early_steps[3]()
    late_steps[3]()

    line_done(r.r_out, S.line_out)
    total = (r.r_out[0].astype(F32) + r.r_out[1].astype(F32)) + (
        r.r_out[2].astype(F32) + r.r_out[3].astype(F32)
    )
    o_gout[...] = total
    squares = total * total
    squares = jnp.sum(squares[:, 0:128] + squares[:, 128:256] + squares[:, 256:384]
                      + squares[:, 384:512] + squares[:, 512:640] + squares[:, 640:768],
                      axis=0, keepdims=True)

    def fold(value):
        total = value[:, 0:128] * value[:, 0:128]
        for t in range(1, value.shape[1] // 128):
            total += value[:, 128 * t : 128 * t + 128] * value[:, 128 * t : 128 * t + 128]
        return jnp.sum(total, axis=0, keepdims=True)

    got(S.slice_in, r.u_in)
    r.t_in[...] = r.u_in[...].astype(F32)
    for p in range(4):
        squares += fold(r.t_in[p])
    trade(r.t_in, r.f_in, S.last_in)
    got(S.line_attn, r.r_attn)
    r.t_attn[0] = (r.r_attn[0].astype(F32) + r.r_attn[1].astype(F32)) + (
        r.r_attn[2].astype(F32) + r.r_attn[3].astype(F32)
    )
    squares += fold(r.t_attn[0])
    trade(r.t_attn, r.f_attn, S.last_attn)
    by_core(lambda columns, width: got(S.line_qkv, r.r_qkv.at[:, :, 0:width]))
    r.t_qkv[...] = r.r_qkv[...].astype(F32)
    trade(r.t_qkv, r.f_qkv, S.last_qkv)
    for p in range(4):
        squares += fold(r.t_qkv[p])
    r.sq[me] = squares

    def send_sq(k):
        other = lax.rem(me + k, ALL)
        push(r.sq.at[me], r.sq.at[me], S.sq, lax.div(other, SEQ), lax.rem(other, SEQ))

    loop(ALL, send_sq, 1)
    sent(S.sq, r.sq.at[0:31])
    got(S.last_in, r.f_in.at[:, 0])
    got(S.last_attn, r.f_attn.at[:, 0])
    for h in range(2):
        for p in range(4):
            value = r.f_in[p, h]
            o_gin[:, 768 * p + 384 * h : 768 * p + 384 * h + 384] = value
        value = r.f_attn[0, h]
        o_gattn[:, 384 * h : 384 * h + 384] = value
    got(S.last_qkv, r.f_qkv.at[:, 0])
    where = {which: index for index, which in enumerate(HALVES) if which is not None}

    def packed_half(chunk, high):
        kind, rest = chunk // 12, chunk % 12
        index = where[(kind, rest % 3)]
        t = index // 2
        tile = r.f_qkv[rest // 3, t // 3, :, t % 3 * 128 : t % 3 * 128 + 128]
        return tile if index % 2 == high else pltpu.roll(tile, 64, 1)

    for t in range(18):
        o_gqkv[:, 128 * t : 128 * t + 128] = jnp.where(
            low, packed_half(2 * t, 0), packed_half(2 * t + 1, 1)
        )
    got(S.early + 3, r.early_all.at[0])
    got(S.late + 3, r.late_all.at[0])
    early_rows = [early_steps[4](k) for k in range(4)]
    late_rows = [late_steps[4](k) for k in range(4)]
    mods = []
    for k in range(4):
        early, late = early_rows[k], late_rows[k]
        rows = jnp.concatenate([late[1:3], early[1:5], jnp.zeros((2, 768), F32)], axis=0)
        for n in range(6):
            for m in range(6):
                r.dmod_flat[k, 6 * n + m : 6 * n + m + 1, :] = rows[
                    n : n + 1, 128 * m : 128 * m + 128
                ]
        mods.append(rows)
    gain = jnp.concatenate(
        [
            sum(late_rows[k][0:1] for k in range(4)),
            sum(early_rows[k][0:1] for k in range(4)),
            (mods[0] + mods[1] + mods[2] + mods[3])[0:6],
        ],
        axis=0,
    )
    mask_row = sum(late_rows[k][3:4] for k in range(4))
    gains = jnp.concatenate([gain, mask_row, jnp.zeros((7, 768), F32)], axis=0)
    masters = jnp.concatenate([i_vec[...], jnp.zeros((7, 768), F32)], axis=0)
    own = lax.rem(WIDTH - 24 * me, WIDTH)
    o_gvec[...] = pltpu.roll(gains, own, 1)[:, 0:128]
    o_vec[...] = pltpu.roll(masters, own, 1)[:, 0:128]
    r.mod_pad[...] = jnp.zeros((8, 384), F32)
    window = lax.div(wide * me, 128)
    for k in range(4):
        rows = r.dmod_flat[k, pl.ds(window, 3), :]
        for m in range(3):
            r.mod_pad[k : k + 1, 128 * m : 128 * m + 128] = rows[m : m + 1, :]
    o_dmod[...] = pltpu.roll(r.mod_pad[...], lax.rem(384 - lax.rem(wide * me, 128), 384), 1)[:, 0:256]
    small = jnp.sum(gain * gain) + jnp.sum(mask_row * mask_row)
    conds = [r.conds_all[k][0:1].astype(BF).astype(F32) for k in range(4)]
    for k in range(4):
        for m in range(k, 4):
            term = jnp.sum(mods[k] * mods[m]) * jnp.sum(conds[k] * conds[m])
            small += term if m == k else 2.0 * term
    got(S.sq, r.sq.at[0:31])
    total = r.sq[0]
    for k in range(1, ALL):
        total += r.sq[k]
    o_norm[...] = jnp.broadcast_to(jnp.sqrt(jnp.sum(total) + small), (8, 128))

    for drained in drains:
        drained()


def run_layer(*args):
    shapes = (
        ((ROWS, WIDTH), BF),
        ((ROWS, WIDTH), F32),
        ((8, 128), F32),
        ((24, 3 * WIDTH), F32),
        ((24, WIDTH), F32),
        ((24, 4 * WIDTH), F32),
        ((96, WIDTH), F32),
        ((8, 256), F32),
        ((16, 128), F32),
        ((16, 128), F32),
        ((8, 128), F32),
    )
    whole = pl.BlockSpec(memory_space=pltpu.VMEM)
    return pl.pallas_call(
        layer_kernel,
        out_shape=[jax.ShapeDtypeStruct(shape, kind) for shape, kind in shapes],
        in_specs=[pl.BlockSpec(memory_space=pl.ANY)] * len(args),
        out_specs=[whole] * len(shapes),
        scratch_shapes=[pltpu.VMEM(shape, kind) for shape, kind in SCRATCH.values()]
        + [pltpu.SMEM((3, 1), jnp.int32)]
        + [pltpu.SemaphoreType.DMA((SEM_COUNT,)), pltpu.SemaphoreType.DMA((SEM_COUNT,))],
        compiler_params=pltpu.CompilerParams(
            collective_id=0, has_side_effects=True, vmem_limit_bytes=60 * 1024 * 1024
        ),
    )(*args)


HELD = (2, 8, 9, 7, 10, 3, 4, 5, 6)


def finish_kernel(*refs):
    sources, outs, refs = refs[:28], refs[28:49], refs[49:]
    near, results, load_sems, store_sems = refs[:28], refs[28:46], refs[46], refs[47]
    norm, g_vec, own_vec, dmod, conds = near[:5]
    weights, moments = (own_vec, *near[9:14]), near[14:26]

    order = list(range(5)) + [14, 15, 9, 16, 17]
    for k in range(2, 6):
        order += [3 + k, 8 + k, 14 + 2 * k, 15 + 2 * k]
    loads = {}
    for n in order:
        source = sources[HELD[n]] if n < 9 else sources[n + 2]
        loads[n] = pltpu.make_async_copy(source, near[n], load_sems.at[n])
        loads[n].start()
    for n in (26, 27):
        loads[n] = pltpu.make_async_copy(sources[n - 26], near[n], load_sems.at[n])
        loads[n].start()
    for n in order[:10]:
        loads[n].wait()
    outs[2][0, 0] = norm[0, 0]
    clip = jnp.minimum(1.0, CLIP / (norm[0:1, 0:1] + 1e-06))
    wide, narrow = near[9].shape[0], moments[0].shape[1]
    rounded = conds[...].astype(BF).astype(F32)
    turned_mod = dmod[...].T
    g_ada = turned_mod[0:wide, 0:1] * rounded[0:1, :]
    for k in range(1, 4):
        g_ada += turned_mod[0:wide, k : k + 1] * rounded[k : k + 1, :]
    stores = []
    for k in range(6):
        if k > 1:
            for n in order[2 + 4 * k : 6 + 4 * k]:
                loads[n].wait()
        grad = g_vec[0:9, 0:narrow] if k == 0 else g_ada if k == 1 else near[3 + k][...]
        updated = adam_step(
            weights[k][...] if k else own_vec[0:9, 0:narrow],
            grad * clip,
            moments[2 * k][...],
            moments[2 * k + 1][...],
            RATE if k else RATE_VECTORS,
            DECAY if k else 0.0,
        )
        for n in range(3):
            at = 3 * k + n
            results[at][...] = updated[n]
            stores.append(pltpu.make_async_copy(results[at], outs[3 + at], store_sems.at[at]))
            stores[-1].start()
    for n in (26, 27):
        loads[n].wait()
        stores.append(pltpu.make_async_copy(near[n], outs[n - 26].at[0], store_sems.at[n - 8]))
        stores[-1].start()
    for copy in stores:
        copy.wait()


def run_finish(partial_results, weights, moments):
    shapes = [((1, ROWS, WIDTH), BF), ((1, ROWS, WIDTH), F32), ((1, 1), F32)]
    for moment in moments[::2]:
        shapes += [(moment.shape, F32)] * 3
    far = pl.BlockSpec(memory_space=pl.ANY)
    specs = [far] * len(shapes)
    specs[2] = pl.BlockSpec(memory_space=pltpu.SMEM)
    near = [partial_results[k] for k in HELD] + [*weights, *moments, *partial_results[:2]]
    args = (*partial_results, *weights, *moments)
    return pl.pallas_call(
        finish_kernel,
        out_shape=[jax.ShapeDtypeStruct(shape, kind) for shape, kind in shapes],
        in_specs=[far] * len(args),
        out_specs=specs,
        scratch_shapes=[pltpu.VMEM(array.shape, array.dtype) for array in near]
        + [pltpu.VMEM(shape, kind) for shape, kind in shapes[3:]]
        + [pltpu.SemaphoreType.DMA((28,)), pltpu.SemaphoreType.DMA((20,))],
        compiler_params=pltpu.CompilerParams(vmem_limit_bytes=60 * 1024 * 1024),
    )(*args)


def slices(
    tokens_in,
    cotangent,
    timesteps,
    span_start,
    span_len,
    vectors,
    w_ada,
    w_qkv,
    w_attn,
    w_in,
    w_out,
    m_vec,
    v_vec,
    m_ada,
    v_ada,
    m_qkv,
    v_qkv,
    m_attn,
    v_attn,
    m_in,
    v_in,
    m_out,
    v_out,
):
    partial_results = run_layer(
        timesteps,
        span_start,
        span_len,
        tokens_in,
        cotangent,
        vectors,
        w_ada.T,
        w_qkv,
        w_attn,
        w_in,
        w_out,
    )
    moments = (
        m_vec,
        v_vec,
        m_ada.T,
        v_ada.T,
        m_qkv,
        v_qkv,
        m_attn,
        v_attn,
        m_in,
        v_in,
        m_out,
        v_out,
    )
    results = run_finish(partial_results, (w_ada.T, w_qkv, w_attn, w_in, w_out), moments)
    ada_results = [result.T for result in results[6:9]]
    return (*results[:2], results[2].reshape(()), *results[3:6], *ada_results, *results[9:])


def solution(mesh):
    in_specs = (
        P("dp", "seq", None),
        P("dp", "seq", None),
        P("dp"),
        P("dp"),
        P("dp"),
        P(),
        P(None, ("dp", "seq")),
        P(("dp", "seq"), None),
        P(("dp", "seq"), None),
        P(("dp", "seq"), None),
        P(("dp", "seq"), None),
        P(None, ("dp", "seq")),
        P(None, ("dp", "seq")),
        P(None, ("dp", "seq")),
        P(None, ("dp", "seq")),
        P(("dp", "seq"), None),
        P(("dp", "seq"), None),
        P(("dp", "seq"), None),
        P(("dp", "seq"), None),
        P(("dp", "seq"), None),
        P(("dp", "seq"), None),
        P(("dp", "seq"), None),
        P(("dp", "seq"), None),
    )
    out_specs = (
        P("dp", "seq", None),
        P("dp", "seq", None),
        P(),
        P(None, ("dp", "seq")),
        P(None, ("dp", "seq")),
        P(None, ("dp", "seq")),
        P(None, ("dp", "seq")),
        P(None, ("dp", "seq")),
        P(None, ("dp", "seq")),
        P(("dp", "seq"), None),
        P(("dp", "seq"), None),
        P(("dp", "seq"), None),
        P(("dp", "seq"), None),
        P(("dp", "seq"), None),
        P(("dp", "seq"), None),
        P(("dp", "seq"), None),
        P(("dp", "seq"), None),
        P(("dp", "seq"), None),
        P(("dp", "seq"), None),
        P(("dp", "seq"), None),
        P(("dp", "seq"), None),
    )
    sizes = dict(mesh.shape)
    local = slices if (sizes["dp"], sizes["seq"]) == (4, 8) else plain
    return jax.shard_map(local, mesh=mesh, in_specs=in_specs, out_specs=out_specs, check_vma=False)
```

```python
from functools import partial
import math
from types import SimpleNamespace

import jax
import jax.numpy as jnp
from jax import lax
from jax.experimental import pallas as pl
from jax.experimental.pallas import tpu as pltpu
from jax.sharding import PartitionSpec as P

HD = 64
COND = 128
STEP = 10


BETA_ONE = 0.9
BETA_TWO = 0.999
ADAM_EPS = 1e-08
RATE = 0.1
RATE_VECTORS = 0.3
DECAY = 0.01
CLIP = 1.0
NORM_EPS = 1e-05


def cond_input(timesteps):
    half_cond = COND // 2
    freqs = jnp.exp(jnp.arange(half_cond, dtype=jnp.float32) * (-math.log(10000.0) / half_cond))
    angles = timesteps.astype(jnp.float32)[:, None] * freqs[None, :]
    return jax.nn.silu(jnp.concatenate([jnp.cos(angles), jnp.sin(angles)], axis=1))


def rotary_tables(positions):
    half_head = HD // 2
    inverse = jnp.exp(jnp.arange(half_head, dtype=jnp.float32) * (-math.log(10000.0) / half_head))
    angles = positions.astype(jnp.float32)[:, None] * inverse[None, :]
    return (jnp.cos(angles), jnp.sin(angles))


def rotate(values, cosines, sines):
    half_head = values.shape[-1] // 2
    first = values[..., :half_head]
    second = values[..., half_head:]
    cos_b = cosines[:, None, :]
    sin_b = sines[:, None, :]
    return jnp.concatenate(
        [first * cos_b - second * sin_b, second * cos_b + first * sin_b], axis=-1
    )


def rotate_back(grads, cosines, sines):
    half_head = grads.shape[-1] // 2
    first = grads[..., :half_head]
    second = grads[..., half_head:]
    cos_b = cosines[:, None, :]
    sin_b = sines[:, None, :]
    return jnp.concatenate(
        [first * cos_b + second * sin_b, second * cos_b - first * sin_b], axis=-1
    )


def normalize(values):
    centre = jnp.mean(values, axis=-1, keepdims=True)
    centred = values - centre
    inverse = lax.rsqrt(jnp.mean(centred * centred, axis=-1, keepdims=True) + NORM_EPS)
    return (centred * inverse, inverse)


def norm_back(normed, inverse, grad):
    return inverse * (
        grad
        - jnp.mean(grad, axis=-1, keepdims=True)
        - normed * jnp.mean(grad * normed, axis=-1, keepdims=True)
    )


def split_kv(block, width):
    seqs, block_rows = (block.shape[0], block.shape[1])
    keys = block[..., :width].reshape(seqs, block_rows, width // HD, HD)
    values = block[..., width:].reshape(seqs, block_rows, width // HD, HD)
    return (keys, values)


def attend_piece(carry, piece, queries, width, factor):
    piece_rows = piece.shape[1]
    size = math.gcd(piece_rows, 512)

    def attend_one_block(index, state):
        running, denom, accum = state
        block = lax.dynamic_slice_in_dim(piece, index * size, size, 1)
        keys, values = split_kv(block, width)
        scores = (
            jnp.einsum("sqhd,skhd->shqk", queries, keys, preferred_element_type=jnp.float32)
            * factor
        )
        highest = jnp.maximum(running, jnp.max(scores, axis=-1))
        shrink = jnp.exp(running - highest)
        weights = jnp.exp(scores - highest[..., None])
        denom = denom * shrink + jnp.sum(weights, axis=-1)
        accum = accum * shrink[..., None] + jnp.einsum(
            "shqk,skhd->shqd",
            weights.astype(jnp.bfloat16),
            values,
            preferred_element_type=jnp.float32,
        )
        return (highest, denom, accum)

    return lax.fori_loop(0, piece_rows // size, attend_one_block, carry)


def block_grads(block, queries, grad_out, logsum, delta, width, factor):
    keys, values = split_kv(block, width)
    scores = (
        jnp.einsum("sqhd,skhd->shqk", queries, keys, preferred_element_type=jnp.float32) * factor
    )
    probs = jnp.exp(scores - logsum[..., None])
    dprobs = jnp.einsum("sqhd,skhd->shqk", grad_out, values, preferred_element_type=jnp.float32)
    dscores = (probs * (dprobs - delta[..., None])).astype(jnp.bfloat16)
    return (keys, probs, dscores)


def query_grads(kv_all, queries, grad_out, logsum, delta, width, factor):
    total_rows = kv_all.shape[1]
    size = math.gcd(total_rows, 512)

    def query_one_block(index, accum):
        block = lax.dynamic_slice_in_dim(kv_all, index * size, size, 1)
        keys, probs, dscores = block_grads(block, queries, grad_out, logsum, delta, width, factor)
        return accum + factor * jnp.einsum(
            "shqk,skhd->sqhd", dscores, keys, preferred_element_type=jnp.float32
        )

    return lax.fori_loop(
        0, total_rows // size, query_one_block, jnp.zeros(queries.shape, jnp.float32)
    )


def key_grads(kv_all, queries, grad_out, logsum, delta, width, factor, count):
    size = math.gcd(count, 512)
    seqs = queries.shape[0]

    def key_one_block(index, accum):
        block = lax.dynamic_slice_in_dim(kv_all, index * size, size, 1)
        keys, probs, dscores = block_grads(block, queries, grad_out, logsum, delta, width, factor)
        grad_vals = jnp.einsum(
            "shqk,sqhd->skhd",
            probs.astype(jnp.bfloat16),
            grad_out,
            preferred_element_type=jnp.float32,
        )
        grad_keys = factor * jnp.einsum(
            "shqk,sqhd->skhd", dscores, queries, preferred_element_type=jnp.float32
        )
        joined = jnp.concatenate(
            [grad_keys.reshape(seqs, size, width), grad_vals.reshape(seqs, size, width)], axis=-1
        )
        return lax.dynamic_update_slice_in_dim(
            accum, jnp.transpose(joined, (1, 0, 2)), index * size, 0
        )

    initial = jnp.zeros((count, seqs, 2 * width), jnp.float32)
    return lax.fori_loop(0, count // size, key_one_block, initial)


def adam_step(weight, grad, first, second, rate, decay_rate):
    new_first = BETA_ONE * first + (1.0 - BETA_ONE) * grad
    new_second = BETA_TWO * second + (1.0 - BETA_TWO) * grad * grad
    fixed_first = new_first / (1.0 - BETA_ONE**STEP)
    fixed_second = new_second / (1.0 - BETA_TWO**STEP)
    new_weight = weight - rate * (
        fixed_first / (jnp.sqrt(fixed_second) + ADAM_EPS) + decay_rate * weight
    )
    return (new_first, new_second, new_weight)


def mod_back(grad_hidden, ln_values, normed, scale_part, gain):
    grad_shift = jnp.sum(grad_hidden, axis=1)
    grad_scale = jnp.sum(grad_hidden * ln_values, axis=1)
    grad_ln = grad_hidden * (1.0 + scale_part)
    grad_gain = jnp.sum(grad_ln * normed, axis=(0, 1))
    return (grad_shift, grad_scale, grad_gain, grad_ln * gain)


def plain(
    tokens_in,
    cotangent,
    timesteps,
    span_start,
    span_len,
    vectors,
    w_ada,
    w_qkv,
    w_attn,
    w_in,
    w_out,
    m_vec,
    v_vec,
    m_ada,
    v_ada,
    m_qkv,
    v_qkv,
    m_attn,
    v_attn,
    m_in,
    v_in,
    m_out,
    v_out,
):
    seqs, group, width = tokens_in.shape
    heads = width // HD
    factor = HD ** (-0.5)
    flat_rows = seqs * group
    full_ada, full_qkv, full_attn, full_in, full_out = (
        lax.all_gather(w_ada.astype(jnp.bfloat16), ("dp", "seq"), axis=1, tiled=True),
        lax.all_gather(w_qkv.astype(jnp.bfloat16), ("dp", "seq"), axis=0, tiled=True),
        lax.all_gather(w_attn.astype(jnp.bfloat16), ("dp", "seq"), axis=0, tiled=True),
        lax.all_gather(w_in.astype(jnp.bfloat16), ("dp", "seq"), axis=0, tiled=True),
        lax.all_gather(w_out.astype(jnp.bfloat16), ("dp", "seq"), axis=0, tiled=True),
    )
    positions = lax.axis_index("seq") * group + jnp.arange(group, dtype=jnp.int32)
    masked = (positions[None, :] >= span_start[:, None]) & (
        positions[None, :] < (span_start + span_len)[:, None]
    )
    cond_bf = cond_input(timesteps).astype(jnp.bfloat16)
    modulation = jnp.dot(cond_bf, full_ada, preferred_element_type=jnp.float32) + vectors[
        2:8
    ].reshape(1, 6 * width)
    pieces = [modulation[:, which * width : (which + 1) * width][:, None, :] for which in range(6)]
    shift_one, scale_one, gate_one, shift_two, scale_two, gate_two = pieces
    start_tokens = jnp.where(
        masked[..., None], vectors[8][None, None, :], tokens_in.astype(jnp.float32)
    )
    normed_one, inv_one = normalize(start_tokens)
    ln_one = normed_one * vectors[0]
    hidden_one = (
        (ln_one * (1.0 + scale_one) + shift_one).astype(jnp.bfloat16).reshape(flat_rows, width)
    )
    projected = jnp.dot(hidden_one, full_qkv, preferred_element_type=jnp.float32).reshape(
        seqs, group, 3 * width
    )
    cosines, sines = rotary_tables(positions)
    queries = rotate(projected[..., :width].reshape(seqs, group, heads, HD), cosines, sines).astype(
        jnp.bfloat16
    )
    keys_here = rotate(
        projected[..., width : 2 * width].reshape(seqs, group, heads, HD), cosines, sines
    ).astype(jnp.bfloat16)
    values_here = projected[..., 2 * width :].astype(jnp.bfloat16)
    kv_local = jnp.concatenate([keys_here.reshape(seqs, group, width), values_here], axis=-1)
    initial = (
        jnp.full((seqs, heads, group), -1e30, jnp.float32),
        jnp.zeros((seqs, heads, group), jnp.float32),
        jnp.zeros((seqs, heads, group, HD), jnp.float32),
    )
    running, denom, accum = attend_piece(
        initial, lax.all_gather(kv_local, "seq", axis=1, tiled=True), queries, width, factor
    )
    attn_heads = accum / denom[..., None]
    logsum = running + jnp.log(denom)
    attn_rows = jnp.transpose(attn_heads, (0, 2, 1, 3)).reshape(flat_rows, width)
    attn_bf = attn_rows.astype(jnp.bfloat16)
    branch_one = jnp.dot(attn_bf, full_attn, preferred_element_type=jnp.float32).reshape(
        seqs, group, width
    )
    mid_tokens = start_tokens + gate_one * branch_one
    normed_two, inv_two = normalize(mid_tokens)
    ln_two = normed_two * vectors[1]
    hidden_two = (
        (ln_two * (1.0 + scale_two) + shift_two).astype(jnp.bfloat16).reshape(flat_rows, width)
    )
    pre_act = jnp.dot(hidden_two, full_in, preferred_element_type=jnp.float32)
    activ, gelu_back = jax.vjp(partial(jax.nn.gelu, approximate=True), pre_act)
    activ_bf = activ.astype(jnp.bfloat16)
    branch_two = jnp.dot(activ_bf, full_out, preferred_element_type=jnp.float32).reshape(
        seqs, group, width
    )
    block_out = (mid_tokens + gate_two * branch_two).astype(jnp.bfloat16)
    grad_y = cotangent.astype(jnp.float32)
    grad_gate_two = jnp.sum(grad_y * branch_two, axis=1)
    grad_branch_two = (grad_y * gate_two).astype(jnp.bfloat16).reshape(flat_rows, width)
    grad_w_out = jnp.dot(activ_bf.T, grad_branch_two, preferred_element_type=jnp.float32)
    grad_activ = jnp.dot(grad_branch_two, full_out.T, preferred_element_type=jnp.float32)
    grad_pre = gelu_back(grad_activ)[0].astype(jnp.bfloat16)
    grad_w_in = jnp.dot(hidden_two.T, grad_pre, preferred_element_type=jnp.float32)
    grad_hidden_two = jnp.dot(grad_pre, full_in.T, preferred_element_type=jnp.float32).reshape(
        seqs, group, width
    )
    grad_shift_two, grad_scale_two, grad_gain_two, grad_normed_two = mod_back(
        grad_hidden_two, ln_two, normed_two, scale_two, vectors[1]
    )
    grad_mid = grad_y + norm_back(normed_two, inv_two, grad_normed_two)
    grad_gate_one = jnp.sum(grad_mid * branch_one, axis=1)
    grad_branch_one = (grad_mid * gate_one).astype(jnp.bfloat16).reshape(flat_rows, width)
    grad_w_attn = jnp.dot(attn_bf.T, grad_branch_one, preferred_element_type=jnp.float32)
    grad_attn_bf = (
        jnp.dot(grad_branch_one, full_attn.T, preferred_element_type=jnp.float32)
        .astype(jnp.bfloat16)
        .reshape(seqs, group, heads, HD)
    )
    delta = jnp.einsum("sqhd,shqd->shq", grad_attn_bf.astype(jnp.float32), attn_heads)
    kv_all = lax.all_gather(kv_local, "seq", axis=1, tiled=True)
    grad_queries = query_grads(kv_all, queries, grad_attn_bf, logsum, delta, width, factor)
    grad_kv = jnp.transpose(
        lax.psum_scatter(
            key_grads(
                kv_all,
                queries,
                grad_attn_bf,
                logsum,
                delta,
                width,
                factor,
                group * lax.axis_size("seq"),
            ).astype(jnp.bfloat16),
            "seq",
            scatter_dimension=0,
            tiled=True,
        ).astype(jnp.float32),
        (1, 0, 2),
    )
    grad_keys = grad_kv[..., :width].reshape(seqs, group, heads, HD)
    grad_qkv = jnp.concatenate(
        [
            rotate_back(grad_queries, cosines, sines).reshape(seqs, group, width),
            rotate_back(grad_keys, cosines, sines).reshape(seqs, group, width),
            grad_kv[..., width:],
        ],
        axis=-1,
    )
    grad_qkv = grad_qkv.astype(jnp.bfloat16).reshape(flat_rows, 3 * width)
    grad_w_qkv = jnp.dot(hidden_one.T, grad_qkv, preferred_element_type=jnp.float32)
    grad_hidden_one = jnp.dot(grad_qkv, full_qkv.T, preferred_element_type=jnp.float32).reshape(
        seqs, group, width
    )
    grad_shift_one, grad_scale_one, grad_gain_one, grad_normed_one = mod_back(
        grad_hidden_one, ln_one, normed_one, scale_one, vectors[0]
    )
    grad_start = grad_mid + norm_back(normed_one, inv_one, grad_normed_one)
    grad_mask_row = jnp.sum(jnp.where(masked[..., None], grad_start, 0.0), axis=(0, 1))
    grad_input = jnp.where(masked[..., None], 0.0, grad_start)
    grad_mod = jnp.concatenate(
        [
            grad_shift_one,
            grad_scale_one,
            grad_gate_one,
            grad_shift_two,
            grad_scale_two,
            grad_gate_two,
        ],
        axis=1,
    )
    grad_w_ada = jnp.dot(cond_bf.astype(jnp.float32).T, grad_mod, precision=lax.Precision.HIGHEST)
    grad_vectors = jnp.concatenate(
        [
            grad_gain_one[None, :],
            grad_gain_two[None, :],
            jnp.sum(grad_mod, axis=0).reshape(6, width),
            grad_mask_row[None, :],
        ],
        axis=0,
    )
    red_ada, red_qkv, red_attn, red_in, red_out, red_vec = (
        lax.psum_scatter(grad_w_ada, ("dp", "seq"), scatter_dimension=1, tiled=True),
        lax.psum_scatter(grad_w_qkv, ("dp", "seq"), scatter_dimension=0, tiled=True),
        lax.psum_scatter(grad_w_attn, ("dp", "seq"), scatter_dimension=0, tiled=True),
        lax.psum_scatter(grad_w_in, ("dp", "seq"), scatter_dimension=0, tiled=True),
        lax.psum_scatter(grad_w_out, ("dp", "seq"), scatter_dimension=0, tiled=True),
        lax.psum_scatter(grad_vectors, ("dp", "seq"), scatter_dimension=1, tiled=True),
    )
    local_squares = jnp.float32(0.0)
    for reduced in (red_vec, red_ada, red_qkv, red_attn, red_in, red_out):
        local_squares = local_squares + jnp.sum(reduced * reduced)
    grad_norm = jnp.sqrt(lax.psum(local_squares, ("dp", "seq")))
    clip_factor = jnp.minimum(1.0, CLIP / (grad_norm + 1e-06))
    columns = red_vec.shape[1]
    own_vectors = lax.dynamic_slice_in_dim(
        vectors, lax.axis_index(("dp", "seq")) * columns, columns, 1
    )
    vec_out = adam_step(own_vectors, red_vec * clip_factor, m_vec, v_vec, RATE_VECTORS, 0.0)
    ada_out = adam_step(w_ada, red_ada * clip_factor, m_ada, v_ada, RATE, DECAY)
    qkv_out = adam_step(w_qkv, red_qkv * clip_factor, m_qkv, v_qkv, RATE, DECAY)
    attn_out = adam_step(w_attn, red_attn * clip_factor, m_attn, v_attn, RATE, DECAY)
    in_out = adam_step(w_in, red_in * clip_factor, m_in, v_in, RATE, DECAY)
    out_out = adam_step(w_out, red_out * clip_factor, m_out, v_out, RATE, DECAY)
    return (
        block_out,
        grad_input,
        grad_norm,
        vec_out[0],
        vec_out[1],
        vec_out[2],
        ada_out[0],
        ada_out[1],
        ada_out[2],
        qkv_out[0],
        qkv_out[1],
        qkv_out[2],
        attn_out[0],
        attn_out[1],
        attn_out[2],
        in_out[0],
        in_out[1],
        in_out[2],
        out_out[0],
        out_out[1],
        out_out[2],
    )


F32, BF = jnp.float32, jnp.bfloat16
MESH = pl.DeviceIdType.MESH
DP, LINE, SEQ, CHIPS, ALL = 4, 4, 8, 16, 32
ROWS, WIDTH, PACK = 128, 768, 640
HALF = WIDTH // 2
HALVES = ((0, 0), (0, 1), (0, 2), (2, 2), (1, 0), (1, 1), (1, 2), None, (2, 0), (2, 1))

def numbered(**counts):
    at = {}
    for name, count in counts.items():
        at[name] = sum(counts[other] for other in at)
    return SimpleNamespace(**at), sum(counts.values())


S, SEM_COUNT = numbered(
    load=11,
    cond=1,
    mix_qkv=1,
    mix_in=1,
    mix_attn=1,
    mod=1,
    w_qkv=1,
    w_attn=4,
    plane_in=1,
    w_in=4,
    w_out=4,
    group_qkv=4,
    group_attn=4,
    fw_qkv=1,
    fw_attn=1,
    fw_in=1,
    fw_out=1,
    tok=4,
    h2=4,
    dm=4,
    xf=4,
    o=1,
    mm=1,
    dh2=1,
    do=1,
    gp=1,
    dh1=5,
    pair_out=1,
    pair_in=1,
    pair_attn=1,
    pair_qkv=1,
    plane_attn=1,
    plane_qkv=1,
    line_out=5,
    line_in=5,
    slice_in=1,
    line_attn=1,
    line_qkv=1,
    last_in=1,
    last_attn=1,
    last_qkv=1,
    early=7,
    late=7,
    sq=1,
)

SCRATCH = dict(
    i_tok=((1, 128, 768), BF),
    i_cot=((1, 128, 768), BF),
    i_vec=((9, 768), F32),
    i_wada=((144, 128), F32),
    i_wqkv=((24, 2304), F32),
    i_wattn=((24, 768), F32),
    i_win=((24, 3072), F32),
    i_wout=((96, 768), F32),
    wide_qkv=((48, 3072), F32),
    wide_in=((48, 3072), F32),
    wide_attn=((48, 768), F32),
    s_qkv=((48, 3072), BF),
    s_in=((48, 3072), BF),
    s_attn=((48, 768), BF),
    w_qkv=((768, 768), BF),
    w_in=((4, 4, 48, 768), BF),
    w_attn=((768, 768), BF),
    w_out=((4, 2, 96, 768), BF),
    t_w_qkv=((640, 768), BF),
    t_w_attn=((768, 1024), BF),
    t_w_in=((768, 768), BF),
    t_w_out=((768, 768), BF),
    t_h1=((768, 512), BF),
    conds_all=((4, 8, 128), F32),
    mod_send=((4, 4, 128), F32),
    mod_got=((32, 4, 128), F32),
    mod_flat=((40, 128), F32),
    mod_pad=((8, 384), F32),
    turn=((2, 4, 128, 128), F32),
    dmod_flat=((4, 40, 128), F32),
    mod=((8, 768), F32),
    x0=((128, 768), F32),
    n1=((4, 128, 768), F32),
    inv1=((4, 128, 128), F32),
    x1=((128, 768), F32),
    n2=((128, 768), F32),
    inv2=((128, 128), F32),
    a=((128, 768), F32),
    dx1=((128, 768), F32),
    toks=((4, 128, 768), BF),
    h1=((4, 128, 768), BF),
    h2=((4, 128, 768), BF),
    dm=((4, 128, 768), BF),
    gb=((4, 128, 768), BF),
    du=((4, 128, 768), BF),
    xb=((2, 4, 128, 640), BF),
    pt=((3, 1024, 512), BF),
    vt=((2, 128, 1024), BF),
    kt=((2, 128, 1024), BF),
    back=((4, 128, 768), F32),
    ot=((2, 128, 512), F32),
    os=((4, 192, 128), BF),
    ob=((4, 192, 128), BF),
    o2=((4, 128, 128), BF),
    mms=((4, 128, 768), BF),
    mmr=((4, 128, 768), BF),
    dhs=((4, 128, 768), BF),
    dhr=((4, 128, 768), BF),
    das=((128, 768), BF),
    dos=((4, 192, 128), BF),
    dob=((4, 192, 128), BF),
    dst=((3, 1024, 512), BF),
    ga=((512, 640), F32),
    gps=((512, 512), BF),
    gpr=((512, 512), BF),
    dqkv=((4, 128, 768), BF),
    d1s=((4, 128, 768), BF),
    d1r=((4, 128, 768), BF),
    g_out=((4, 2, 96, 768), BF),
    g_in=((2, 4, 4, 48, 384), BF),
    g_attn=((2, 768, 384), BF),
    g_qkv=((2, 768, 384), BF),
    p_out=((4, 96, 768), BF),
    p_in=((4, 4, 48, 384), BF),
    p_attn=((768, 384), BF),
    p_qkv=((768, 384), BF),
    q_attn=((4, 192, 384), BF),
    q_qkv=((4, 192, 384), BF),
    m_attn=((192, 384), BF),
    m_qkv=((192, 384), BF),
    r_out=((4, 96, 768), BF),
    r_in=((4, 4, 48, 384), BF),
    via_in=((4, 48, 384), BF),
    via_out=((96, 768), BF),
    via_dh1=((128, 768), BF),
    m_in=((4, 48, 384), BF),
    u_in=((4, 48, 384), BF),
    r_attn=((4, 48, 384), BF),
    r_qkv=((4, 48, 384), BF),
    t_in=((4, 48, 384), F32),
    t_attn=((1, 48, 384), F32),
    t_qkv=((4, 48, 384), F32),
    f_in=((4, 2, 24, 384), F32),
    f_attn=((1, 2, 24, 384), F32),
    f_qkv=((4, 2, 24, 384), F32),
    early=((8, 768), F32),
    early_pair=((8, 768), F32),
    early_line=((4, 8, 384), F32),
    early_plane=((4, 8, 384), F32),
    early_all=((2, 4, 8, 384), F32),
    late=((4, 768), F32),
    late_pair=((4, 768), F32),
    late_line=((4, 4, 384), F32),
    late_plane=((4, 4, 384), F32),
    late_all=((2, 4, 4, 384), F32),
    sq=((32, 1, 128), F32),
)


def dot(left, right):
    return jnp.dot(left, right, preferred_element_type=F32)


def dot_nt(left, right):
    return lax.dot_general(left, right, (((1,), (1,)), ((), ())), preferred_element_type=F32)


def dot_tn(left, right):
    return lax.dot_general(left, right, (((0,), (0,)), ((), ())), preferred_element_type=F32)


def loop(count, body, start=0):
    def step(index, carry):
        body(index)
        return carry

    lax.fori_loop(start, count, step, 0)


def layer_kernel(
    i_time,
    i_start,
    i_len,
    h_tok,
    h_cot,
    h_vec,
    h_wada,
    h_wqkv,
    h_wattn,
    h_win,
    h_wout,
    o_y,
    o_dx,
    o_norm,
    o_gqkv,
    o_gattn,
    o_gin,
    o_gout,
    o_dmod,
    o_gvec,
    o_vec,
    o_conds,
    *scratch,
):
    r = SimpleNamespace(**dict(zip(SCRATCH, scratch)), when=scratch[-3])
    send_sems, recv_sems = scratch[-2:]
    i_tok, i_cot, i_vec, i_wada = r.i_tok, r.i_cot, r.i_vec, r.i_wada
    i_wqkv, i_wattn, i_win, i_wout = r.i_wqkv, r.i_wattn, r.i_win, r.i_wout
    b, s = lax.axis_index("dp"), lax.axis_index("seq")
    z, c = lax.div(s, 2), lax.rem(s, 2)
    mate = s + 1 - 2 * c
    chip = b * LINE + z
    me = b * SEQ + s
    drains = []

    def push(src, dst, at, to_b, to_s, out=None):
        pltpu.make_async_remote_copy(
            src_ref=src,
            dst_ref=dst,
            send_sem=send_sems.at[at if out is None else out],
            recv_sem=recv_sems.at[at],
            device_id=(to_b, to_s),
            device_id_type=MESH,
        ).start()

    def keep(src, dst, at):
        pltpu.make_async_copy(src, dst, recv_sems.at[at]).start()

    def got(at, like):
        pltpu.make_async_copy(like, like, recv_sems.at[at]).wait()

    def left(at, like):
        pltpu.make_async_copy(like, like, send_sems.at[at]).wait()

    def sent(at, like):
        drains.append(lambda: left(at, like))

    def by_core(body):
        for h, width in ((0, HALF), (1, PACK - HALF)):

            @pl.when(c == h)
            def _():
                body(slice(HALF * h, HALF * h + width), width)

    def sent_by_core(at, like):
        drains.append(lambda: by_core(lambda columns, width: left(at, like(width))))

    near = (b, b + 1 - 2 * lax.rem(b, 2), b + 2 - 4 * lax.div(b, 2), 3 - b)

    def toward(k):
        if k == 3:
            return 3, near[3]
        slot = 1 + c if k == 1 else 2 - c
        return slot, (1 - c) * near[k] + c * near[3 - k]

    def peers(body):
        for k in (1, 2, 3):
            body(*toward(k))

    def stack(body):
        for k in (1, 2, 3):
            body(lax.rem(z + k + 2 * c * (2 - k), LINE))

    def line_gather(block, at, near=True, rest=True):
        inner = 1 + lax.rem(z, 2)
        if near:
            push(block(z), block(z), at + z, b, 2 * inner + c, at)

        def one(to):
            relayed = ((z == 1) & (to == 3)) | ((z == 2) & (to == 0))

            @pl.when(jnp.logical_not(relayed | (to == inner)))
            def _():
                push(block(z), block(z), at + z, b, 2 * to + c, at)

        if rest:
            stack(one)

    def line_relay(block, at):
        for middle, source, to in ((2, 1, 3), (1, 2, 0)):

            @pl.when(z == middle)
            def _():
                got(at + source, block(source))
                push(block(source), block(source), at + source, b, 2 * to + c, at)

    def line_got(block, at, k):
        here = (k == z) | ((z == 2) & (k == 1)) | ((z == 1) & (k == 2))

        @pl.when(jnp.logical_not(here))
        def _():
            got(at + k, block(0))

    far = lax.div(z, 2)

    def line_order(j):
        return lax.rem(z + (2, 3 - 2 * far, 1 + 2 * far, 0)[j], LINE)

    def line_add(j, rows, dst, via, at):
        to = line_order(j)
        outer_chip = (z == 0) | (z == 3)

        def direct():
            push(rows(to), dst.at[z], at + z, b, 2 * to + c, at)

        if j == 0:

            @pl.when(outer_chip)
            def _():
                push(rows(to), via, at + 4, b, 2 * (1 + far) + c, at)

            @pl.when(jnp.logical_not(outer_chip))
            def _():
                direct()

        elif j < 3:
            direct()
        else:
            keep(rows(z), dst.at[z], at + z)

    def line_via(via, at, add):
        @pl.when((z == 1) | (z == 2))
        def _():
            got(at + 4, via)
            add()

    def line_done(dst, at):
        for k in range(4):
            missing = ((z == 1) & (k == 3)) | ((z == 2) & (k == 0))

            @pl.when(jnp.logical_not(missing))
            def _():
                got(at + k, dst.at[k])

    def line_clear(dst):
        for middle, k in ((1, 3), (2, 0)):

            @pl.when(z == middle)
            def _():
                dst[k] = jnp.zeros(dst.shape[1:], BF)

    lane = lax.broadcasted_iota(jnp.int32, (1, 128), 1)
    low = lane < 64
    own24 = pl.ds(pl.multiple_of(24 * c, 8), 24)
    mate24 = pl.ds(pl.multiple_of(24 * (1 - c), 8), 24)
    part = pl.ds(pl.multiple_of(HALF * c, 128), HALF)
    chip_rows = pl.ds(pl.multiple_of(48 * chip, 16), 48)
    group_rows = pl.ds(pl.multiple_of(192 * b, 16), 192)

    barrier = pltpu.get_barrier_semaphore()

    def greet(k):
        other = lax.rem(me + k, ALL)
        pl.semaphore_signal(
            barrier, inc=1, device_id=(lax.div(other, SEQ), lax.rem(other, SEQ)), device_id_type=MESH
        )

    loads = (
        (i_time, r.when.at[0]),
        (i_start, r.when.at[1]),
        (i_len, r.when.at[2]),
        (h_wqkv, i_wqkv),
        (h_win, i_win),
        (h_wattn, i_wattn),
        (h_wout, i_wout),
        (h_tok, i_tok),
        (h_vec, i_vec),
        (h_wada, i_wada),
        (h_cot, i_cot),
    )
    for k, (src, dst) in enumerate(loads):
        pltpu.make_async_copy(src, dst, recv_sems.at[S.load + k]).start()
    loop(ALL, greet, 1)
    for k, (src, dst) in enumerate(loads):
        pltpu.make_async_copy(src, dst, recv_sems.at[S.load + k]).wait()

    def natural(kind, p, head):
        return kind * WIDTH + 192 * p + 64 * head

    def half_at(ref, column, high):
        tile = ref[:, column // 128 * 128 : column // 128 * 128 + 128]
        return tile if (column % 128 == 64) == high else pltpu.roll(tile, 64, 1)

    for p in range(4):
        for tile in range(5):
            pair = []
            for high in (0, 1):
                which = HALVES[2 * tile + high]
                pair.append(
                    jnp.zeros((24, 128), F32)
                    if which is None
                    else half_at(i_wqkv, natural(which[0], p, which[1]), bool(high))
                )
            r.wide_qkv[own24, 768 * p + 128 * tile : 768 * p + 128 * tile + 128] = jnp.where(
                low, pair[0], pair[1]
            )
        r.wide_qkv[own24, 768 * p + 640 : 768 * p + 768] = jnp.zeros((24, 128), F32)
    r.wide_in[own24, :] = i_win[...]
    r.wide_attn[own24, :] = i_wattn[...]
    r.w_out[z, c] = i_wout[...].astype(BF)
    r.toks[z] = i_tok[0]
    line_clear(r.r_out)
    line_clear(r.r_in)
    line_clear(r.d1r)
    for ref in (r.q_qkv, r.r_qkv):
        ref[:, :, PACK - HALF : HALF] = jnp.zeros((4, ref.shape[1], WIDTH - PACK), BF)
    lanes8 = lax.broadcasted_iota(jnp.int32, (8, 128), 1)
    half_cond = COND // 2
    speed = jnp.exp((lanes8 % half_cond).astype(F32) * (-math.log(10000.0) / half_cond))
    angle = r.when[0, 0].astype(F32) * speed
    wave = jnp.where(lanes8 < half_cond, jnp.cos(angle), jnp.sin(angle))
    r.conds_all[b] = wave * (1.0 / (1.0 + jnp.exp(-wave)))
    pl.semaphore_wait(barrier, ALL - 1)

    def token_block(k):
        return r.toks.at[k]

    def attn_block(k):
        return r.w_attn.at[pl.ds(pl.multiple_of(192 * b + 48 * k, 16), 48), part]

    def in_block(k):
        return r.w_in.at[:, k, :, part]

    def out_block(k):
        return r.w_out.at[k, c]

    peers(lambda k, to: push(r.conds_all.at[b], r.conds_all.at[b], S.cond, to, s))
    sent(S.cond, r.conds_all.at[0:3])
    push(r.wide_qkv.at[own24], r.wide_qkv.at[own24], S.mix_qkv, b, mate)
    sent(S.mix_qkv, r.wide_qkv.at[0:24])
    push(r.wide_attn.at[own24], r.wide_attn.at[own24], S.mix_attn, b, mate)
    sent(S.mix_attn, r.wide_attn.at[0:24])
    push(r.wide_in.at[own24], r.wide_in.at[own24], S.mix_in, b, mate)
    sent(S.mix_in, r.wide_in.at[0:24])

    got(S.cond, r.conds_all.at[0:3])
    row8 = lax.broadcasted_iota(jnp.int32, (8, 128), 0)
    cond4 = jnp.zeros((8, 128), F32)
    for k in range(4):
        cond4 = jnp.where(row8 == k, r.conds_all[k], cond4)
    o_conds[...] = cond4
    wide = i_wada.shape[0]
    r.mod_pad[...] = jnp.zeros((8, 384), F32)
    r.mod_pad[:, 0:wide] = dot_nt(cond4.astype(BF), i_wada[...].astype(BF))
    columns = pltpu.roll(r.mod_pad[...], lax.rem(wide * me, 128), 1)
    for k in range(4):
        for t in range(3):
            r.mod_send[k, t : t + 1, :] = columns[k : k + 1, 128 * t : 128 * t + 128]
        r.mod_send[k, 3:4, :] = jnp.zeros((1, 128), F32)

    def send_mod(k):
        other = lax.rem(me + k, ALL)
        ob = lax.div(other, SEQ)
        push(r.mod_send.at[ob], r.mod_got.at[me], S.mod, ob, lax.rem(other, SEQ))

    loop(ALL, send_mod, 1)
    sent(S.mod, r.mod_got.at[0:31])
    keep(r.mod_send.at[b], r.mod_got.at[me], S.mod)

    def block(src, first):
        return src.at[:, pl.ds(pl.multiple_of(first, 128), HALF)]

    def slices_along_line():
        def send(columns, width):
            def rows(to):
                first = pl.multiple_of(WIDTH * to + columns.start, 128)
                return r.s_qkv.at[:, pl.ds(first, width)]

            dst = r.w_qkv.at[chip_rows, columns]
            stack(lambda to: push(rows(to), dst, S.w_qkv, b, 2 * to + c))
            keep(rows(z), dst, S.w_qkv)

        by_core(send)
        sent_by_core(S.w_qkv, lambda width: r.w_qkv.at[0:144, 0:width])

    def over_plane(dst, at):
        rows = dst.at[group_rows, part]
        peers(lambda k, to: push(rows, rows, at + k, to, s))
        for k in (1, 2, 3):
            sent(at + k, dst.at[0:192, 0:HALF])

    def share(dst, at, onward):
        for k in range(4):
            rows = dst.at[pl.ds(pl.multiple_of(192 * near[k], 16), 192), part]
            if k:
                got(at + k, rows)
            push(rows, rows, onward, b, mate)
        sent(onward, dst.at[:, 0:HALF])

    def line_share(block, at, onward):
        for k in range(4):
            line_got(block, at, k)
            push(block(k), block(k), onward, b, mate)

    got(S.mix_qkv, r.wide_qkv.at[0:24])
    r.s_qkv[...] = r.wide_qkv[...].astype(BF)
    slices_along_line()
    line_gather(token_block, S.tok, rest=False)
    sent(S.tok, r.toks.at[0:3])
    got(S.mix_attn, r.wide_attn.at[0:24])
    r.s_attn[...] = r.wide_attn[...].astype(BF)

    def qkv_over_plane(columns, width):
        got(S.w_qkv, r.w_qkv.at[0:192, 0:width])
        rows = r.w_qkv.at[group_rows, columns]
        peers(lambda k, to: push(rows, rows, S.group_qkv + k, to, s))

    by_core(qkv_over_plane)
    for k in (1, 2, 3):
        sent_by_core(S.group_qkv + k, lambda width: r.w_qkv.at[0:192, 0:width])
    line_gather(token_block, S.tok, near=False)
    for h in range(2):

        @pl.when(c == h)
        def _():
            r.w_attn[chip_rows, 384 * h : 384 * h + 384] = r.s_attn[:, 384 * h : 384 * h + 384]

    line_gather(attn_block, S.w_attn)
    sent(S.w_attn, r.w_attn.at[0:144, 0:HALF])
    line_gather(out_block, S.w_out)
    sent(S.w_out, r.w_out.at[0:3, 0])
    got(S.mix_in, r.wide_in.at[0:24])
    r.s_in[...] = r.wide_in[...].astype(BF)
    peers(
        lambda k, to: push(
            block(r.s_in, WIDTH * to + HALF * c), r.w_in.at[b, z, :, part], S.plane_in, to, s
        )
    )
    keep(block(r.s_in, WIDTH * b + HALF * c), r.w_in.at[b, z, :, part], S.plane_in)
    sent(S.plane_in, r.w_in.at[0:3, 0, :, 0:HALF])

    def hidden_rows(k):
        place = (2 * k + c) * ROWS + lax.broadcasted_iota(jnp.int32, (ROWS, 1), 0)
        return (place >= r.when[1, 0]) & (place < r.when[1, 0] + r.when[2, 0])

    def first_norm(tokens, k):
        x0 = jnp.where(hidden_rows(k), i_vec[8:9, :], tokens.astype(F32))
        normed, inverse = normalize(x0)
        r.n1[k] = normed
        r.inv1[k] = jnp.broadcast_to(inverse, (ROWS, 128))
        return x0

    r.x0[...] = first_norm(i_tok[0], z)

    got(S.mod, r.mod_got)
    r.mod_flat[...] = jnp.zeros((40, 128), F32)
    for k in range(ALL):
        first = 9 * k // 8
        r.mod_flat[first : first + 3, :] += r.mod_got[k, 0:3, :]
    for k in range(6):
        row = jnp.concatenate(
            [r.mod_flat[6 * k + t : 6 * k + t + 1, :] for t in range(6)], axis=1
        )
        r.mod[k : k + 1, :] = row + i_vec[2 + k : 3 + k, :]

    def mod(k):
        return r.mod[k : k + 1, :]

    def vec(k):
        return i_vec[k : k + 1, :]

    r.h1[z] = (r.n1[z] * vec(0) * (1.0 + mod(1)) + mod(0)).astype(BF)
    r.dm[0] = (i_cot[0].astype(F32) * mod(5)).astype(BF)
    peers(lambda k, to: push(r.dm.at[0], r.dm.at[k], S.dm + k, to, s))
    for k in (1, 2, 3):
        sent(S.dm + k, r.dm.at[0])

    lanes = lax.broadcasted_iota(jnp.int32, (ROWS, 128), 1)
    first_half = lanes % HD < HD // 2
    speed = jnp.exp((lanes % (HD // 2)).astype(F32) * (-math.log(10000.0) / (HD // 2)))
    row = lax.broadcasted_iota(jnp.int32, (ROWS, 128), 0)

    def table(k):
        angle = ((2 * k + c) * ROWS + row).astype(F32) * speed
        r.turn[0, k] = jnp.cos(angle)
        sine = jnp.sin(angle)
        r.turn[1, k] = jnp.where(first_half, -sine, sine)

    loop(LINE, table)

    line_relay(token_block, S.tok)

    def qkv_share(columns, width):
        for k in range(4):
            rows = r.w_qkv.at[pl.ds(pl.multiple_of(192 * near[k], 16), 192), columns]
            if k:
                got(S.group_qkv + k, rows)
            push(rows, rows, S.fw_qkv, b, mate)

    by_core(qkv_share)
    sent_by_core(S.fw_qkv, lambda width: r.w_qkv.at[:, 0:width])
    by_core(lambda columns, width: got(S.fw_qkv, r.w_qkv.at[:, 0 : PACK - width]))
    for k in range(5):
        columns = slice(128 * k, 128 * k + 128)
        r.t_w_qkv[columns, :] = r.w_qkv[:, columns].T

    def turned(tile, sign, k):
        other = jnp.where(first_half, pltpu.roll(tile, 96, 1), pltpu.roll(tile, 32, 1))
        return tile * r.turn[0, k] + sign * (other * r.turn[1, k])

    def project(j):
        k = lax.rem(z + j, LINE)

        @pl.when(j > 0)
        def _():
            line_got(token_block, S.tok, k)
            first_norm(r.toks[k], k)
            r.h1[k] = (r.n1[k] * vec(0) * (1.0 + mod(1)) + mod(0)).astype(BF)

        x = dot(r.h1[k], r.w_qkv[:, 0:PACK])
        tiles = [x[:, 128 * t : 128 * t + 128] for t in range(5)]
        tiles[0] = turned(tiles[0], 1.0, k) * 0.125
        tiles[1] = jnp.where(low, turned(tiles[1], 1.0, k) * 0.125, tiles[1])
        tiles[2] = turned(tiles[2], 1.0, k)
        tiles[3] = turned(tiles[3], 1.0, k)
        for t in range(5):
            r.xb[0, k, :, 128 * t : 128 * t + 128] = tiles[t].astype(BF)
        push(r.xb.at[0, k], r.xb.at[1, k], S.xf + k, b, mate)

    loop(4, project)
    line_relay(attn_block, S.w_attn)
    for k in range(4):
        line_got(attn_block, S.w_attn, k)
    over_plane(r.w_attn, S.group_attn)
    for k in range(4):
        sent(S.xf + k, r.xb.at[0, 0])

    for k in range(6):
        columns = slice(128 * k, 128 * k + 128)
        r.t_h1[columns, :] = r.h1[:, :, columns].reshape(512, 128).T
    for k in range(4):
        got(S.xf + k, r.xb.at[0, 0])

    def tile_of(t):
        return r.xb[:, :, :, 128 * t : 128 * t + 128].reshape(1024, 128)

    heads = ((0, 2, 4, True, True), (0, 2, 4, False, False), (1, 3, 1, True, False))

    def queries(head, first, size):
        q_tile, _, _, q_low, _ = heads[head]
        q = r.xb[0, first : first + size, :, 128 * q_tile : 128 * q_tile + 128]
        return jnp.where(low if q_low else ~low, q.reshape(size * 128, 128), jnp.zeros((), BF))

    r.vt[0] = tile_of(4).T
    r.vt[1] = tile_of(1).T
    for half in range(2):
        at = slice(256 * half, 256 * half + 256)
        for head in range(3):
            scores = dot_nt(tile_of(heads[head][1]), queries(head, 2 * half, 2))
            weights = jnp.exp(scores - jnp.max(scores, axis=0, keepdims=True))
            weights = weights * (1.0 / jnp.sum(weights, axis=0, keepdims=True))
            weights = weights.astype(BF)
            r.pt[head, :, at] = weights
            out = dot(r.vt[head // 2], weights)
            if head == 0:
                r.ot[0, 0:64, at] = out[0:64]
            elif head == 1:
                r.ot[0, 64:128, at] = out[64:128]
            else:
                r.ot[1, 0:64, at] = out[64:128]
                r.ot[1, 64:128, at] = jnp.zeros((64, 256), F32)
        for k in (2 * half, 2 * half + 1):
            across = slice(128 * k, 128 * k + 128)
            r.os[k, 0:128, :] = r.ot[0, :, across].T.astype(BF)
            third = r.ot[1, 0:64, across]
            third = jnp.concatenate([third, pltpu.roll(third, 64, 1)], axis=0)
            r.os[k, 128:192, :] = third.T[0:64].astype(BF)
        for to in (2 * half, 2 * half + 1):

            @pl.when(z == to)
            def _():
                keep(r.os.at[to], r.ob.at[z], S.o)

            @pl.when(z != to)
            def _():
                push(r.os.at[to], r.ob.at[z], S.o, b, 2 * to + c)

        if half == 0:
            line_relay(out_block, S.w_out)

    sent(S.o, r.os.at[0:3])
    got(S.plane_in, r.w_in.at[:, 0, :, 0:HALF])
    line_gather(in_block, S.w_in)
    sent(S.w_in, r.w_in.at[0:3, :, :, 0:HALF])
    for k in range(2):
        r.kt[k] = tile_of(2 + k).T
    share(r.w_attn, S.group_attn, S.fw_attn)
    got(S.fw_attn, r.w_attn.at[:, 0:HALF])
    for p in range(4):
        first = 192 * p
        r.t_w_attn[:, 256 * p : 256 * p + 128] = r.w_attn[first : first + 128, :].T
        third = r.w_attn[first + 128 : first + 192, :]
        r.t_w_attn[:, 256 * p + 128 : 256 * p + 256] = jnp.concatenate(
            [third, jnp.zeros_like(third)], axis=0
        ).T
    got(S.o, r.ob)
    a = jnp.zeros((ROWS, WIDTH), F32)
    for p in range(4):
        third = r.ob[p, 128:192, :].astype(F32)
        third = jnp.concatenate([third, pltpu.roll(third, 64, 1)], axis=0)
        r.o2[p] = jnp.where(low, third, 0.0).astype(BF)
        a += dot(r.ob[p, 0:128, :], r.w_attn[192 * p : 192 * p + 128, :])
        a += dot(r.o2[p, :, 0:64], r.w_attn[192 * p + 128 : 192 * p + 192, :])
    r.a[...] = a
    x1 = r.x0[...] + mod(2) * a
    r.x1[...] = x1
    n2, inv2 = normalize(x1)
    r.n2[...] = n2
    r.inv2[...] = jnp.broadcast_to(inv2, (ROWS, 128))
    r.h2[0] = (n2 * vec(1) * (1.0 + mod(4)) + mod(3)).astype(BF)
    peers(lambda k, to: push(r.h2.at[0], r.h2.at[k], S.h2 + k, to, s))
    for k in (1, 2, 3):
        sent(S.h2 + k, r.h2.at[0])
    line_relay(in_block, S.w_in)
    line_share(out_block, S.w_out, S.fw_out)
    sent(S.fw_out, r.w_out.at[:, 0])
    got(S.fw_out, r.w_out.at[:, 0])

    for k in range(6):
        columns = slice(128 * k, 128 * k + 128)
        r.t_w_out[columns, :] = r.w_out[:, :, :, columns].reshape(WIDTH, 128).T

    def feed_back(k):
        @pl.when(k > 0)
        def _():
            got(S.dm + k, r.dm.at[0])

        r.back[k] = dot(r.dm[k], r.t_w_out[...])

    loop(4, feed_back)
    line_share(in_block, S.w_in, S.fw_in)
    sent(S.fw_in, r.w_in.at[:, :, :, 0:HALF])
    got(S.fw_in, r.w_in.at[:, :, :, 0:HALF])
    for k in range(6):
        columns = slice(128 * k, 128 * k + 128)
        r.t_w_in[columns, :] = r.w_in[:, :, :, columns].reshape(WIDTH, 128).T

    def feed(first, count):
        at = slice(first, first + count)
        size = count * ROWS
        u = dot(r.h2[at].reshape(size, WIDTH), r.w_in[...].reshape(WIDTH, WIDTH))
        slope = 0.7978845608028654
        cube = 0.044715
        t = jnp.tanh(slope * (u + cube * u * u * u))
        r.gb[at] = (0.5 * u * (1.0 + t)).astype(BF).reshape(count, ROWS, WIDTH)
        bend = 0.5 * (1.0 + t) + 0.5 * u * (1.0 - t * t) * (slope * (1.0 + 3.0 * cube * u * u))
        du = (r.back[at].reshape(size, WIDTH) * bend).astype(BF)
        r.du[at] = du.reshape(count, ROWS, WIDTH)
        r.dhs[at] = dot(du, r.t_w_in[...]).astype(BF).reshape(count, ROWS, WIDTH)

    for first, count in ((1, 2), (3, 1)):
        for k in range(first, first + count):
            got(S.h2 + k, r.h2.at[0])
        feed(first, count)
        for k in range(first, first + count):
            slot, to = toward(k)
            push(r.dhs.at[slot], r.dhr.at[slot], S.dh2, to, s)
    sent(S.dh2, r.dhs.at[0:3])
    feed(0, 1)
    def gather(own, others):
        total = own[0].astype(F32)
        for k in (1, 2, 3):
            total += others[k].astype(F32)
        return total

    for k in range(2):
        rows = slice(384 * k, 384 * k + 384)
        result = dot_tn(r.gb[:, :, rows].reshape(512, 384), r.dm[...].reshape(512, 768))
        r.g_out[2 * k : 2 * k + 2] = result.astype(BF).reshape(2, 2, 96, 768)
    push(r.g_out.at[:, 1 - c], r.p_out, S.pair_out, b, mate)
    sent(S.pair_out, r.p_out)

    def to_mate(grad, dst, at):
        push(grad.at[1 - c], dst, at, b, mate)
        sent(at, dst)

    def pair_sum(grad, pair, at):
        got(at, pair)
        grad[c] = (grad[c].astype(F32) + pair[...].astype(F32)).astype(BF)

    def plane_sum(grad, dst, at, packed=False):
        def send(columns, width):
            def rows(to):
                return grad.at[c, pl.ds(pl.multiple_of(192 * to, 16), 192), 0:width]

            peers(lambda k, to: push(rows(to), dst.at[k, :, 0:width], at, to, s))
            keep(rows(b), dst.at[0, :, 0:width], at)

        if packed:
            by_core(send)
            sent_by_core(at, lambda width: dst.at[0:3, :, 0:width])
        else:
            send(None, HALF)
            sent(at, dst.at[0:3])

    def line_sum(src, total, dst, first, at, packed=False):
        def send(columns, width):
            got(first, src.at[:, :, 0:width])
            total[...] = (
                (src[0].astype(F32) + src[1].astype(F32))
                + (src[2].astype(F32) + src[3].astype(F32))
            ).astype(BF)

            def rows(to):
                return total.at[pl.ds(pl.multiple_of(48 * to, 16), 48), 0:width]

            stack(lambda to: push(rows(to), dst.at[z, :, 0:width], at, b, 2 * to + c))
            keep(rows(z), dst.at[z, :, 0:width], at)

        if packed:
            by_core(send)
            sent_by_core(at, lambda width: dst.at[0:3, :, 0:width])
        else:
            send(None, HALF)
            sent(at, dst.at[0:3])

    def trade(total, final, at):
        push(total.at[:, mate24], final.at[:, c], at, b, mate)
        sent(at, final.at[:, 0])
        final[:, c] = total[:, own24, :]

    def in_product(k):
        rows = slice(384 * k, 384 * k + 384)
        result = dot_tn(r.h2[:, :, rows].reshape(512, 384), r.du[...].reshape(512, 768)).astype(BF)
        for h in range(2):
            r.g_in[h, 2 * k : 2 * k + 2] = result[:, 384 * h : 384 * h + 384].reshape(2, 4, 48, 384)

    in_product(0)

    got(S.pair_out, r.p_out)
    for k in range(4):
        r.g_out[k, c] = (r.g_out[k, c].astype(F32) + r.p_out[k].astype(F32)).astype(BF)

    def out_rows(k):
        return r.g_out.at[k, c]

    for j in (0, 1):
        line_add(j, out_rows, r.r_out, r.via_out, S.line_out)
    in_product(1)
    to_mate(r.g_in, r.p_in, S.pair_in)

    def add_out():
        k = line_order(2)
        r.g_out[k, c] = (r.g_out[k, c].astype(F32) + r.via_out[...].astype(F32)).astype(BF)

    got(S.dh2, r.dhr.at[0:3])
    dh = gather(r.dhs, r.dhr)
    n2 = r.n2[...]
    inv2 = r.inv2[:, 0:1]
    r.early[...] = jnp.zeros((8, 768), F32)
    r.early[2:3, :] = jnp.sum(dh, axis=0, keepdims=True)
    both = jnp.sum(dh * n2, axis=0, keepdims=True)
    r.early[3:4, :] = both * vec(1)
    r.early[0:1, :] = both * (1.0 + mod(4))
    grad = dh * ((1.0 + mod(4)) * vec(1))
    dx1 = i_cot[0].astype(F32) + norm_back(n2, inv2, grad)
    r.dx1[...] = dx1
    r.early[1:2, :] = jnp.sum(dx1 * r.a[...], axis=0, keepdims=True)
    r.das[...] = (dx1 * mod(2)).astype(BF)
    for p in range(4):
        result = dot(r.das[...], r.t_w_attn[:, 256 * p : 256 * p + 256])
        r.dos[p, 0:128, :] = result[:, 0:128].astype(BF)
        third = result[:, 128:256]
        third = jnp.where(low, third[0:64], pltpu.roll(third[64:128], 64, 1))
        r.dos[p, 128:192, :] = third.astype(BF)
    stack(lambda to: push(r.dos.at[to], r.dob.at[z], S.do, b, 2 * to + c))
    keep(r.dos.at[z], r.dob.at[z], S.do)
    sent(S.do, r.dos.at[0:3])
    for t in range(3):
        at = slice(256 * t, 256 * t + 256)
        mm = dot(r.gb[...].reshape(512, WIDTH), r.w_out[:, :, :, at].reshape(WIDTH, 256))
        r.mms[:, :, at] = mm.astype(BF).reshape(4, ROWS, 256)
    peers(lambda k, to: push(r.mms.at[k], r.mmr.at[k], S.mm, to, s))
    sent(S.mm, r.mms.at[0:3])

    for p in range(4):
        for rows, left_side in (
            (slice(192 * p, 192 * p + 128), r.ob[p, 0:128, :]),
            (slice(192 * p + 128, 192 * p + 192), r.o2[p]),
        ):
            result = dot_tn(left_side, r.das[...])[0 : rows.stop - rows.start].astype(BF)
            r.g_attn[0, rows, :] = result[:, 0:HALF]
            r.g_attn[1, rows, :] = result[:, HALF:WIDTH]
    to_mate(r.g_attn, r.p_attn, S.pair_attn)

    def small_sum(src, pair, line, plane, whole, at):
        def first():
            push(src, pair, at, b, mate)
            sent(at, src)

        def second():
            got(at, pair)
            total = src[...] + pair[...]
            line[z] = (1 - c) * total[:, 0:HALF] + c * total[:, HALF:WIDTH]
            stack(lambda to: push(line.at[z], line.at[z], at + 1, b, 2 * to + c))
            sent(at + 1, line.at[0:3])

        def third():
            got(at + 1, line.at[0:3])
            plane[b] = (line[0] + line[1]) + (line[2] + line[3])
            peers(lambda k, to: push(plane.at[b], plane.at[b], at + 2, to, s))
            sent(at + 2, plane.at[0:3])

        def fourth():
            got(at + 2, plane.at[0:3])
            whole[c] = plane[...]
            push(plane, whole.at[c], at + 3, b, mate)
            sent(at + 3, plane)

        def rows(k):
            return jnp.concatenate([whole[0, k], whole[1, k]], axis=1)

        return first, second, third, fourth, rows

    early_steps = small_sum(
        r.early, r.early_pair, r.early_line, r.early_plane, r.early_all, S.early
    )
    late_steps = small_sum(r.late, r.late_pair, r.late_line, r.late_plane, r.late_all, S.late)

    pair_sum(r.g_in, r.p_in, S.pair_in)
    line_via(r.via_out, S.line_out, add_out)
    for j in (2, 3):
        line_add(j, out_rows, r.r_out, r.via_out, S.line_out)
    sent(S.line_out, r.r_out.at[0:3])

    def in_rows(k):
        return r.g_in.at[c, :, k]

    for j in (0, 1):
        line_add(j, in_rows, r.r_in, r.via_in, S.line_in)

    def add_in():
        k = line_order(2)
        r.g_in[c, :, k] = (r.g_in[c, :, k].astype(F32) + r.via_in[...].astype(F32)).astype(BF)

    pair_sum(r.g_attn, r.p_attn, S.pair_attn)
    plane_sum(r.g_attn, r.q_attn, S.plane_attn)

    got(S.do, r.dob)
    dot0 = r.dob[:, 0:128, :].reshape(512, 128)
    third = r.dob[:, 128:192, :].astype(F32).reshape(256, 128)
    other_rows = jnp.where(low, pltpu.roll(third, 64, 1), 0.0).reshape(4, 64, 128)
    third = jnp.where(low, third, 0.0).reshape(4, 64, 128)
    dot1 = jnp.concatenate([third, other_rows], axis=1).reshape(512, 128)
    zero = jnp.zeros((), BF)
    moved = pltpu.roll(dot1, 64, 1).astype(BF)
    grads = (jnp.where(low, dot0, zero), jnp.where(low, zero, dot0), moved)
    product = dot0.astype(F32).T * r.ot[0]
    deltas = (
        jnp.sum(product[0:64], axis=0, keepdims=True),
        jnp.sum(product[64:128], axis=0, keepdims=True),
        jnp.sum(dot1.T * r.ot[1], axis=0, keepdims=True),
    )
    for head in range(3):
        values = tile_of(heads[head][2])
        for half in range(2):
            at = slice(256 * half, 256 * half + 256)
            dp = dot_nt(values, grads[head][at])
            r.dst[head, :, at] = (
                r.pt[head, :, at].astype(F32) * (dp - deltas[head][:, at])
            ).astype(BF)

    def key_grads(rows):
        dk = [dot(r.dst[head, rows, :], queries(head, 0, 4)) for head in range(3)]
        dv = [dot(r.pt[head, rows, :], grads[head]) for head in range(3)]
        return (dv[2], dk[0] + dk[1], dk[2], dv[0] + dv[1])

    line_via(r.via_in, S.line_in, add_in)
    for j in (2, 3):
        line_add(j, in_rows, r.r_in, r.via_in, S.line_in)
    sent(S.line_in, r.r_in.at[0:3])
    for t, tile in enumerate(key_grads(slice(512, 1024))):
        r.gps[:, 128 * t : 128 * t + 128] = tile.astype(BF)
    push(r.gps, r.gpr, S.gp, b, mate)
    sent(S.gp, r.gps)
    for t, tile in enumerate(key_grads(slice(0, 512))):
        r.ga[:, 128 * t + 128 : 128 * t + 256] = tile
    for half in range(2):
        at = slice(256 * half, 256 * half + 256)
        turned_q = [dot(r.kt[head // 2], r.dst[head, :, at]) for head in range(3)]
        top = jnp.concatenate([turned_q[0][0:64], turned_q[1][64:128]], axis=0)
        r.ga[at, 0:128] = top.T * 0.125
        r.ga[at, 128:256] += turned_q[2].T * 0.125
    got(S.gp, r.gpr)

    def dh1_rows(k):
        return r.d1s.at[k]

    def back_turn(k):
        rows = pl.ds(pl.multiple_of(128 * k, 128), 128)
        tiles = [r.ga[rows, 0:128]] + [
            r.ga[rows, 128 * t : 128 * t + 128]
            + r.gpr[rows, 128 * t - 128 : 128 * t].astype(F32)
            for t in range(1, 5)
        ]
        tiles[0] = turned(tiles[0], -1.0, k)
        tiles[1] = jnp.where(low, turned(tiles[1], -1.0, k), tiles[1])
        tiles[2] = turned(tiles[2], -1.0, k)
        tiles[3] = turned(tiles[3], -1.0, k)
        for t in range(5):
            r.dqkv[k, :, 128 * t : 128 * t + 128] = tiles[t].astype(BF)
        r.dqkv[k, :, PACK:WIDTH] = jnp.zeros((128, 128), BF)

    back_turn(line_order(0))

    def unproject(j):
        k = line_order(j)
        partial_sum = dot(r.dqkv[k, :, 0:PACK], r.t_w_qkv[...])
        r.d1s[k] = partial_sum.astype(BF)
        if j == 2:

            def add():
                r.d1s[k] = (partial_sum + r.via_dh1[...].astype(F32)).astype(BF)

            line_via(r.via_dh1, S.dh1, add)
        line_add(j, dh1_rows, r.d1r, r.via_dh1, S.dh1)
        n = r.n1[k]
        e = partial_sum * ((1.0 + mod(1)) * vec(0))
        weight = jnp.where(hidden_rows(k), r.inv1[k][:, 0:1], 0.0)
        centred = (
            e
            - jnp.mean(e, axis=-1, keepdims=True)
            - n * jnp.mean(e * n, axis=-1, keepdims=True)
        )
        r.late[0:1, :] += jnp.sum(partial_sum * n, axis=0, keepdims=True)
        r.late[1:2, :] += jnp.sum(partial_sum, axis=0, keepdims=True)
        r.late[3:4, :] += jnp.sum(weight * centred, axis=0, keepdims=True)

    r.late[...] = jnp.zeros((4, 768), F32)
    r.late[3:4, :] = jnp.sum(
        jnp.where(hidden_rows(z), r.dx1[...], 0.0), axis=0, keepdims=True
    )
    unproject(0)
    for j in (1, 2, 3):
        back_turn(line_order(j))

    def qkv_rows(k):
        rows = pl.ds(pl.multiple_of(128 * k, 128), 128)
        result = dot(r.t_h1[rows, :], r.dqkv[...].reshape(512, WIDTH)).astype(BF)
        r.g_qkv[0, rows, :] = result[:, 0:HALF]
        r.g_qkv[1, rows, :] = result[:, HALF:WIDTH]

    loop(6, qkv_rows)
    to_mate(r.g_qkv, r.p_qkv, S.pair_qkv)
    unproject(1)
    pair_sum(r.g_qkv, r.p_qkv, S.pair_qkv)
    plane_sum(r.g_qkv, r.q_qkv, S.plane_qkv, True)
    got(S.mm, r.mmr.at[0:3])
    mm = gather(r.mms, r.mmr)
    o_y[...] = (r.x1[...] + mod(5) * mm).astype(BF)
    r.early[4:5, :] = jnp.sum(i_cot[0].astype(F32) * mm, axis=0, keepdims=True)
    early_steps[0]()
    unproject(2)
    unproject(3)
    sent(S.dh1, r.d1s.at[0:3])
    both = r.late[0:1, :]
    r.late[2:3, :] = both * vec(0)
    r.late[0:1, :] = both * (1.0 + mod(1))
    late_steps[0]()
    early_steps[1]()
    line_sum(r.q_attn, r.m_attn, r.r_attn, S.plane_attn, S.line_attn)
    late_steps[1]()

    line_done(r.r_in, S.line_in)
    r.m_in[...] = (
        (r.r_in[0].astype(F32) + r.r_in[1].astype(F32))
        + (r.r_in[2].astype(F32) + r.r_in[3].astype(F32))
    ).astype(BF)
    peers(lambda k, to: push(r.m_in.at[to], r.u_in.at[b], S.slice_in, to, s))
    keep(r.m_in.at[b], r.u_in.at[b], S.slice_in)
    sent(S.slice_in, r.u_in.at[0:3])
    line_sum(r.q_qkv, r.m_qkv, r.r_qkv, S.plane_qkv, S.line_qkv, True)
    early_steps[2]()
    late_steps[2]()

    line_done(r.d1r, S.dh1)
    dh = (r.d1r[0].astype(F32) + r.d1r[1].astype(F32)) + (
        r.d1r[2].astype(F32) + r.d1r[3].astype(F32)
    )
    n1 = r.n1[z]
    grad = dh * ((1.0 + mod(1)) * vec(0))
    dx0 = r.dx1[...] + norm_back(n1, r.inv1[z][:, 0:1], grad)
    o_dx[...] = jnp.where(hidden_rows(z), 0.0, dx0)
    early_steps[3]()
    late_steps[3]()

    line_done(r.r_out, S.line_out)
    total = (r.r_out[0].astype(F32) + r.r_out[1].astype(F32)) + (
        r.r_out[2].astype(F32) + r.r_out[3].astype(F32)
    )
    o_gout[...] = total
    squares = total * total
    squares = jnp.sum(squares[:, 0:128] + squares[:, 128:256] + squares[:, 256:384]
                      + squares[:, 384:512] + squares[:, 512:640] + squares[:, 640:768],
                      axis=0, keepdims=True)

    def fold(value):
        total = value[:, 0:128] * value[:, 0:128]
        for t in range(1, value.shape[1] // 128):
            total += value[:, 128 * t : 128 * t + 128] * value[:, 128 * t : 128 * t + 128]
        return jnp.sum(total, axis=0, keepdims=True)

    got(S.slice_in, r.u_in)
    r.t_in[...] = r.u_in[...].astype(F32)
    for p in range(4):
        squares += fold(r.t_in[p])
    trade(r.t_in, r.f_in, S.last_in)
    got(S.line_attn, r.r_attn)
    r.t_attn[0] = (r.r_attn[0].astype(F32) + r.r_attn[1].astype(F32)) + (
        r.r_attn[2].astype(F32) + r.r_attn[3].astype(F32)
    )
    squares += fold(r.t_attn[0])
    trade(r.t_attn, r.f_attn, S.last_attn)
    by_core(lambda columns, width: got(S.line_qkv, r.r_qkv.at[:, :, 0:width]))
    r.t_qkv[...] = r.r_qkv[...].astype(F32)
    trade(r.t_qkv, r.f_qkv, S.last_qkv)
    for p in range(4):
        squares += fold(r.t_qkv[p])
    r.sq[me] = squares

    def send_sq(k):
        other = lax.rem(me + k, ALL)
        push(r.sq.at[me], r.sq.at[me], S.sq, lax.div(other, SEQ), lax.rem(other, SEQ))

    loop(ALL, send_sq, 1)
    sent(S.sq, r.sq.at[0:31])
    got(S.last_in, r.f_in.at[:, 0])
    got(S.last_attn, r.f_attn.at[:, 0])
    for h in range(2):
        for p in range(4):
            value = r.f_in[p, h]
            o_gin[:, 768 * p + 384 * h : 768 * p + 384 * h + 384] = value
        value = r.f_attn[0, h]
        o_gattn[:, 384 * h : 384 * h + 384] = value
    got(S.last_qkv, r.f_qkv.at[:, 0])
    where = {which: index for index, which in enumerate(HALVES) if which is not None}

    def packed_half(chunk, high):
        kind, rest = chunk // 12, chunk % 12
        index = where[(kind, rest % 3)]
        t = index // 2
        tile = r.f_qkv[rest // 3, t // 3, :, t % 3 * 128 : t % 3 * 128 + 128]
        return tile if index % 2 == high else pltpu.roll(tile, 64, 1)

    for t in range(18):
        o_gqkv[:, 128 * t : 128 * t + 128] = jnp.where(
            low, packed_half(2 * t, 0), packed_half(2 * t + 1, 1)
        )
    got(S.early + 3, r.early_all.at[0])
    got(S.late + 3, r.late_all.at[0])
    early_rows = [early_steps[4](k) for k in range(4)]
    late_rows = [late_steps[4](k) for k in range(4)]
    mods = []
    for k in range(4):
        early, late = early_rows[k], late_rows[k]
        rows = jnp.concatenate([late[1:3], early[1:5], jnp.zeros((2, 768), F32)], axis=0)
        for n in range(6):
            for m in range(6):
                r.dmod_flat[k, 6 * n + m : 6 * n + m + 1, :] = rows[
                    n : n + 1, 128 * m : 128 * m + 128
                ]
        mods.append(rows)
    gain = jnp.concatenate(
        [
            sum(late_rows[k][0:1] for k in range(4)),
            sum(early_rows[k][0:1] for k in range(4)),
            (mods[0] + mods[1] + mods[2] + mods[3])[0:6],
        ],
        axis=0,
    )
    mask_row = sum(late_rows[k][3:4] for k in range(4))
    gains = jnp.concatenate([gain, mask_row, jnp.zeros((7, 768), F32)], axis=0)
    masters = jnp.concatenate([i_vec[...], jnp.zeros((7, 768), F32)], axis=0)
    own = lax.rem(WIDTH - 24 * me, WIDTH)
    o_gvec[...] = pltpu.roll(gains, own, 1)[:, 0:128]
    o_vec[...] = pltpu.roll(masters, own, 1)[:, 0:128]
    r.mod_pad[...] = jnp.zeros((8, 384), F32)
    window = lax.div(wide * me, 128)
    for k in range(4):
        rows = r.dmod_flat[k, pl.ds(window, 3), :]
        for m in range(3):
            r.mod_pad[k : k + 1, 128 * m : 128 * m + 128] = rows[m : m + 1, :]
    o_dmod[...] = pltpu.roll(r.mod_pad[...], lax.rem(384 - lax.rem(wide * me, 128), 384), 1)[:, 0:256]
    small = jnp.sum(gain * gain) + jnp.sum(mask_row * mask_row)
    conds = [r.conds_all[k][0:1].astype(BF).astype(F32) for k in range(4)]
    for k in range(4):
        for m in range(k, 4):
            term = jnp.sum(mods[k] * mods[m]) * jnp.sum(conds[k] * conds[m])
            small += term if m == k else 2.0 * term
    got(S.sq, r.sq.at[0:31])
    total = r.sq[0]
    for k in range(1, ALL):
        total += r.sq[k]
    o_norm[...] = jnp.broadcast_to(jnp.sqrt(jnp.sum(total) + small), (8, 128))

    for drained in drains:
        drained()


def run_layer(*args):
    shapes = (
        ((ROWS, WIDTH), BF),
        ((ROWS, WIDTH), F32),
        ((8, 128), F32),
        ((24, 3 * WIDTH), F32),
        ((24, WIDTH), F32),
        ((24, 4 * WIDTH), F32),
        ((96, WIDTH), F32),
        ((8, 256), F32),
        ((16, 128), F32),
        ((16, 128), F32),
        ((8, 128), F32),
    )
    whole = pl.BlockSpec(memory_space=pltpu.VMEM)
    return pl.pallas_call(
        layer_kernel,
        out_shape=[jax.ShapeDtypeStruct(shape, kind) for shape, kind in shapes],
        in_specs=[pl.BlockSpec(memory_space=pl.ANY)] * len(args),
        out_specs=[whole] * len(shapes),
        scratch_shapes=[pltpu.VMEM(shape, kind) for shape, kind in SCRATCH.values()]
        + [pltpu.SMEM((3, 1), jnp.int32)]
        + [pltpu.SemaphoreType.DMA((SEM_COUNT,)), pltpu.SemaphoreType.DMA((SEM_COUNT,))],
        compiler_params=pltpu.CompilerParams(
            collective_id=0, has_side_effects=True, vmem_limit_bytes=60 * 1024 * 1024
        ),
    )(*args)


HELD = (2, 8, 9, 7, 10, 3, 4, 5, 6)


def finish_kernel(*refs):
    sources, outs, refs = refs[:28], refs[28:49], refs[49:]
    near, results, load_sems, store_sems = refs[:28], refs[28:46], refs[46], refs[47]
    norm, g_vec, own_vec, dmod, conds = near[:5]
    weights, moments = (own_vec, *near[9:14]), near[14:26]

    order = list(range(5)) + [14, 15, 9, 16, 17]
    for k in range(2, 6):
        order += [3 + k, 8 + k, 14 + 2 * k, 15 + 2 * k]
    loads = {}
    for n in order:
        source = sources[HELD[n]] if n < 9 else sources[n + 2]
        loads[n] = pltpu.make_async_copy(source, near[n], load_sems.at[n])
        loads[n].start()
    for n in (26, 27):
        loads[n] = pltpu.make_async_copy(sources[n - 26], near[n], load_sems.at[n])
        loads[n].start()
    for n in order[:10]:
        loads[n].wait()
    outs[2][0, 0] = norm[0, 0]
    clip = jnp.minimum(1.0, CLIP / (norm[0:1, 0:1] + 1e-06))
    wide, narrow = near[9].shape[0], moments[0].shape[1]
    rounded = conds[...].astype(BF).astype(F32)
    turned_mod = dmod[...].T
    g_ada = turned_mod[0:wide, 0:1] * rounded[0:1, :]
    for k in range(1, 4):
        g_ada += turned_mod[0:wide, k : k + 1] * rounded[k : k + 1, :]
    stores = []
    for k in range(6):
        if k > 1:
            for n in order[2 + 4 * k : 6 + 4 * k]:
                loads[n].wait()
        grad = g_vec[0:9, 0:narrow] if k == 0 else g_ada if k == 1 else near[3 + k][...]
        updated = adam_step(
            weights[k][...] if k else own_vec[0:9, 0:narrow],
            grad * clip,
            moments[2 * k][...],
            moments[2 * k + 1][...],
            RATE if k else RATE_VECTORS,
            DECAY if k else 0.0,
        )
        for n in range(3):
            at = 3 * k + n
            results[at][...] = updated[n]
            stores.append(pltpu.make_async_copy(results[at], outs[3 + at], store_sems.at[at]))
            stores[-1].start()
    for n in (26, 27):
        loads[n].wait()
        stores.append(pltpu.make_async_copy(near[n], outs[n - 26].at[0], store_sems.at[n - 8]))
        stores[-1].start()
    for copy in stores:
        copy.wait()


def run_finish(partial_results, weights, moments):
    shapes = [((1, ROWS, WIDTH), BF), ((1, ROWS, WIDTH), F32), ((1, 1), F32)]
    for moment in moments[::2]:
        shapes += [(moment.shape, F32)] * 3
    far = pl.BlockSpec(memory_space=pl.ANY)
    specs = [far] * len(shapes)
    specs[2] = pl.BlockSpec(memory_space=pltpu.SMEM)
    near = [partial_results[k] for k in HELD] + [*weights, *moments, *partial_results[:2]]
    args = (*partial_results, *weights, *moments)
    return pl.pallas_call(
        finish_kernel,
        out_shape=[jax.ShapeDtypeStruct(shape, kind) for shape, kind in shapes],
        in_specs=[far] * len(args),
        out_specs=specs,
        scratch_shapes=[pltpu.VMEM(array.shape, array.dtype) for array in near]
        + [pltpu.VMEM(shape, kind) for shape, kind in shapes[3:]]
        + [pltpu.SemaphoreType.DMA((28,)), pltpu.SemaphoreType.DMA((20,))],
        compiler_params=pltpu.CompilerParams(vmem_limit_bytes=60 * 1024 * 1024),
    )(*args)


def slices(
    tokens_in,
    cotangent,
    timesteps,
    span_start,
    span_len,
    vectors,
    w_ada,
    w_qkv,
    w_attn,
    w_in,
    w_out,
    m_vec,
    v_vec,
    m_ada,
    v_ada,
    m_qkv,
    v_qkv,
    m_attn,
    v_attn,
    m_in,
    v_in,
    m_out,
    v_out,
):
    partial_results = run_layer(
        timesteps,
        span_start,
        span_len,
        tokens_in,
        cotangent,
        vectors,
        w_ada.T,
        w_qkv,
        w_attn,
        w_in,
        w_out,
    )
    moments = (
        m_vec,
        v_vec,
        m_ada.T,
        v_ada.T,
        m_qkv,
        v_qkv,
        m_attn,
        v_attn,
        m_in,
        v_in,
        m_out,
        v_out,
    )
    results = run_finish(partial_results, (w_ada.T, w_qkv, w_attn, w_in, w_out), moments)
    ada_results = [result.T for result in results[6:9]]
    return (*results[:2], results[2].reshape(()), *results[3:6], *ada_results, *results[9:])


def solution(mesh):
    in_specs = (
        P("dp", "seq", None),
        P("dp", "seq", None),
        P("dp"),
        P("dp"),
        P("dp"),
        P(),
        P(None, ("dp", "seq")),
        P(("dp", "seq"), None),
        P(("dp", "seq"), None),
        P(("dp", "seq"), None),
        P(("dp", "seq"), None),
        P(None, ("dp", "seq")),
        P(None, ("dp", "seq")),
        P(None, ("dp", "seq")),
        P(None, ("dp", "seq")),
        P(("dp", "seq"), None),
        P(("dp", "seq"), None),
        P(("dp", "seq"), None),
        P(("dp", "seq"), None),
        P(("dp", "seq"), None),
        P(("dp", "seq"), None),
        P(("dp", "seq"), None),
        P(("dp", "seq"), None),
    )
    out_specs = (
        P("dp", "seq", None),
        P("dp", "seq", None),
        P(),
        P(None, ("dp", "seq")),
        P(None, ("dp", "seq")),
        P(None, ("dp", "seq")),
        P(None, ("dp", "seq")),
        P(None, ("dp", "seq")),
        P(None, ("dp", "seq")),
        P(("dp", "seq"), None),
        P(("dp", "seq"), None),
        P(("dp", "seq"), None),
        P(("dp", "seq"), None),
        P(("dp", "seq"), None),
        P(("dp", "seq"), None),
        P(("dp", "seq"), None),
        P(("dp", "seq"), None),
        P(("dp", "seq"), None),
        P(("dp", "seq"), None),
        P(("dp", "seq"), None),
        P(("dp", "seq"), None),
    )
    sizes = dict(mesh.shape)
    local = slices if (sizes["dp"], sizes["seq"]) == (4, 8) else plain
    return jax.shard_map(local, mesh=mesh, in_specs=in_specs, out_specs=out_specs, check_vma=False)
```

```python
from functools import partial
import math
from types import SimpleNamespace

import jax
import jax.numpy as jnp
from jax import lax
from jax.experimental import pallas as pl
from jax.experimental.pallas import tpu as pltpu
from jax.sharding import PartitionSpec as P

HD = 64
COND = 128
STEP = 10


BETA_ONE = 0.9
BETA_TWO = 0.999
ADAM_EPS = 1e-08
RATE = 0.1
RATE_VECTORS = 0.3
DECAY = 0.01
CLIP = 1.0
NORM_EPS = 1e-05


def cond_input(timesteps):
    half_cond = COND // 2
    freqs = jnp.exp(jnp.arange(half_cond, dtype=jnp.float32) * (-math.log(10000.0) / half_cond))
    angles = timesteps.astype(jnp.float32)[:, None] * freqs[None, :]
    return jax.nn.silu(jnp.concatenate([jnp.cos(angles), jnp.sin(angles)], axis=1))


def rotary_tables(positions):
    half_head = HD // 2
    inverse = jnp.exp(jnp.arange(half_head, dtype=jnp.float32) * (-math.log(10000.0) / half_head))
    angles = positions.astype(jnp.float32)[:, None] * inverse[None, :]
    return (jnp.cos(angles), jnp.sin(angles))


def rotate(values, cosines, sines):
    half_head = values.shape[-1] // 2
    first = values[..., :half_head]
    second = values[..., half_head:]
    cos_b = cosines[:, None, :]
    sin_b = sines[:, None, :]
    return jnp.concatenate(
        [first * cos_b - second * sin_b, second * cos_b + first * sin_b], axis=-1
    )


def rotate_back(grads, cosines, sines):
    half_head = grads.shape[-1] // 2
    first = grads[..., :half_head]
    second = grads[..., half_head:]
    cos_b = cosines[:, None, :]
    sin_b = sines[:, None, :]
    return jnp.concatenate(
        [first * cos_b + second * sin_b, second * cos_b - first * sin_b], axis=-1
    )


def normalize(values):
    centre = jnp.mean(values, axis=-1, keepdims=True)
    centred = values - centre
    inverse = lax.rsqrt(jnp.mean(centred * centred, axis=-1, keepdims=True) + NORM_EPS)
    return (centred * inverse, inverse)


def norm_back(normed, inverse, grad):
    return inverse * (
        grad
        - jnp.mean(grad, axis=-1, keepdims=True)
        - normed * jnp.mean(grad * normed, axis=-1, keepdims=True)
    )


def split_kv(block, width):
    seqs, block_rows = (block.shape[0], block.shape[1])
    keys = block[..., :width].reshape(seqs, block_rows, width // HD, HD)
    values = block[..., width:].reshape(seqs, block_rows, width // HD, HD)
    return (keys, values)


def attend_piece(carry, piece, queries, width, factor):
    piece_rows = piece.shape[1]
    size = math.gcd(piece_rows, 512)

    def attend_one_block(index, state):
        running, denom, accum = state
        block = lax.dynamic_slice_in_dim(piece, index * size, size, 1)
        keys, values = split_kv(block, width)
        scores = (
            jnp.einsum("sqhd,skhd->shqk", queries, keys, preferred_element_type=jnp.float32)
            * factor
        )
        highest = jnp.maximum(running, jnp.max(scores, axis=-1))
        shrink = jnp.exp(running - highest)
        weights = jnp.exp(scores - highest[..., None])
        denom = denom * shrink + jnp.sum(weights, axis=-1)
        accum = accum * shrink[..., None] + jnp.einsum(
            "shqk,skhd->shqd",
            weights.astype(jnp.bfloat16),
            values,
            preferred_element_type=jnp.float32,
        )
        return (highest, denom, accum)

    return lax.fori_loop(0, piece_rows // size, attend_one_block, carry)


def block_grads(block, queries, grad_out, logsum, delta, width, factor):
    keys, values = split_kv(block, width)
    scores = (
        jnp.einsum("sqhd,skhd->shqk", queries, keys, preferred_element_type=jnp.float32) * factor
    )
    probs = jnp.exp(scores - logsum[..., None])
    dprobs = jnp.einsum("sqhd,skhd->shqk", grad_out, values, preferred_element_type=jnp.float32)
    dscores = (probs * (dprobs - delta[..., None])).astype(jnp.bfloat16)
    return (keys, probs, dscores)


def query_grads(kv_all, queries, grad_out, logsum, delta, width, factor):
    total_rows = kv_all.shape[1]
    size = math.gcd(total_rows, 512)

    def query_one_block(index, accum):
        block = lax.dynamic_slice_in_dim(kv_all, index * size, size, 1)
        keys, probs, dscores = block_grads(block, queries, grad_out, logsum, delta, width, factor)
        return accum + factor * jnp.einsum(
            "shqk,skhd->sqhd", dscores, keys, preferred_element_type=jnp.float32
        )

    return lax.fori_loop(
        0, total_rows // size, query_one_block, jnp.zeros(queries.shape, jnp.float32)
    )


def key_grads(kv_all, queries, grad_out, logsum, delta, width, factor, count):
    size = math.gcd(count, 512)
    seqs = queries.shape[0]

    def key_one_block(index, accum):
        block = lax.dynamic_slice_in_dim(kv_all, index * size, size, 1)
        keys, probs, dscores = block_grads(block, queries, grad_out, logsum, delta, width, factor)
        grad_vals = jnp.einsum(
            "shqk,sqhd->skhd",
            probs.astype(jnp.bfloat16),
            grad_out,
            preferred_element_type=jnp.float32,
        )
        grad_keys = factor * jnp.einsum(
            "shqk,sqhd->skhd", dscores, queries, preferred_element_type=jnp.float32
        )
        joined = jnp.concatenate(
            [grad_keys.reshape(seqs, size, width), grad_vals.reshape(seqs, size, width)], axis=-1
        )
        return lax.dynamic_update_slice_in_dim(
            accum, jnp.transpose(joined, (1, 0, 2)), index * size, 0
        )

    initial = jnp.zeros((count, seqs, 2 * width), jnp.float32)
    return lax.fori_loop(0, count // size, key_one_block, initial)


def adam_step(weight, grad, first, second, rate, decay_rate):
    new_first = BETA_ONE * first + (1.0 - BETA_ONE) * grad
    new_second = BETA_TWO * second + (1.0 - BETA_TWO) * grad * grad
    fixed_first = new_first / (1.0 - BETA_ONE**STEP)
    fixed_second = new_second / (1.0 - BETA_TWO**STEP)
    new_weight = weight - rate * (
        fixed_first / (jnp.sqrt(fixed_second) + ADAM_EPS) + decay_rate * weight
    )
    return (new_first, new_second, new_weight)


def mod_back(grad_hidden, ln_values, normed, scale_part, gain):
    grad_shift = jnp.sum(grad_hidden, axis=1)
    grad_scale = jnp.sum(grad_hidden * ln_values, axis=1)
    grad_ln = grad_hidden * (1.0 + scale_part)
    grad_gain = jnp.sum(grad_ln * normed, axis=(0, 1))
    return (grad_shift, grad_scale, grad_gain, grad_ln * gain)


def plain(
    tokens_in,
    cotangent,
    timesteps,
    span_start,
    span_len,
    vectors,
    w_ada,
    w_qkv,
    w_attn,
    w_in,
    w_out,
    m_vec,
    v_vec,
    m_ada,
    v_ada,
    m_qkv,
    v_qkv,
    m_attn,
    v_attn,
    m_in,
    v_in,
    m_out,
    v_out,
):
    seqs, group, width = tokens_in.shape
    heads = width // HD
    factor = HD ** (-0.5)
    flat_rows = seqs * group
    full_ada, full_qkv, full_attn, full_in, full_out = (
        lax.all_gather(w_ada.astype(jnp.bfloat16), ("dp", "seq"), axis=1, tiled=True),
        lax.all_gather(w_qkv.astype(jnp.bfloat16), ("dp", "seq"), axis=0, tiled=True),
        lax.all_gather(w_attn.astype(jnp.bfloat16), ("dp", "seq"), axis=0, tiled=True),
        lax.all_gather(w_in.astype(jnp.bfloat16), ("dp", "seq"), axis=0, tiled=True),
        lax.all_gather(w_out.astype(jnp.bfloat16), ("dp", "seq"), axis=0, tiled=True),
    )
    positions = lax.axis_index("seq") * group + jnp.arange(group, dtype=jnp.int32)
    masked = (positions[None, :] >= span_start[:, None]) & (
        positions[None, :] < (span_start + span_len)[:, None]
    )
    cond_bf = cond_input(timesteps).astype(jnp.bfloat16)
    modulation = jnp.dot(cond_bf, full_ada, preferred_element_type=jnp.float32) + vectors[
        2:8
    ].reshape(1, 6 * width)
    pieces = [modulation[:, which * width : (which + 1) * width][:, None, :] for which in range(6)]
    shift_one, scale_one, gate_one, shift_two, scale_two, gate_two = pieces
    start_tokens = jnp.where(
        masked[..., None], vectors[8][None, None, :], tokens_in.astype(jnp.float32)
    )
    normed_one, inv_one = normalize(start_tokens)
    ln_one = normed_one * vectors[0]
    hidden_one = (
        (ln_one * (1.0 + scale_one) + shift_one).astype(jnp.bfloat16).reshape(flat_rows, width)
    )
    projected = jnp.dot(hidden_one, full_qkv, preferred_element_type=jnp.float32).reshape(
        seqs, group, 3 * width
    )
    cosines, sines = rotary_tables(positions)
    queries = rotate(projected[..., :width].reshape(seqs, group, heads, HD), cosines, sines).astype(
        jnp.bfloat16
    )
    keys_here = rotate(
        projected[..., width : 2 * width].reshape(seqs, group, heads, HD), cosines, sines
    ).astype(jnp.bfloat16)
    values_here = projected[..., 2 * width :].astype(jnp.bfloat16)
    kv_local = jnp.concatenate([keys_here.reshape(seqs, group, width), values_here], axis=-1)
    initial = (
        jnp.full((seqs, heads, group), -1e30, jnp.float32),
        jnp.zeros((seqs, heads, group), jnp.float32),
        jnp.zeros((seqs, heads, group, HD), jnp.float32),
    )
    running, denom, accum = attend_piece(
        initial, lax.all_gather(kv_local, "seq", axis=1, tiled=True), queries, width, factor
    )
    attn_heads = accum / denom[..., None]
    logsum = running + jnp.log(denom)
    attn_rows = jnp.transpose(attn_heads, (0, 2, 1, 3)).reshape(flat_rows, width)
    attn_bf = attn_rows.astype(jnp.bfloat16)
    branch_one = jnp.dot(attn_bf, full_attn, preferred_element_type=jnp.float32).reshape(
        seqs, group, width
    )
    mid_tokens = start_tokens + gate_one * branch_one
    normed_two, inv_two = normalize(mid_tokens)
    ln_two = normed_two * vectors[1]
    hidden_two = (
        (ln_two * (1.0 + scale_two) + shift_two).astype(jnp.bfloat16).reshape(flat_rows, width)
    )
    pre_act = jnp.dot(hidden_two, full_in, preferred_element_type=jnp.float32)
    activ, gelu_back = jax.vjp(partial(jax.nn.gelu, approximate=True), pre_act)
    activ_bf = activ.astype(jnp.bfloat16)
    branch_two = jnp.dot(activ_bf, full_out, preferred_element_type=jnp.float32).reshape(
        seqs, group, width
    )
    block_out = (mid_tokens + gate_two * branch_two).astype(jnp.bfloat16)
    grad_y = cotangent.astype(jnp.float32)
    grad_gate_two = jnp.sum(grad_y * branch_two, axis=1)
    grad_branch_two = (grad_y * gate_two).astype(jnp.bfloat16).reshape(flat_rows, width)
    grad_w_out = jnp.dot(activ_bf.T, grad_branch_two, preferred_element_type=jnp.float32)
    grad_activ = jnp.dot(grad_branch_two, full_out.T, preferred_element_type=jnp.float32)
    grad_pre = gelu_back(grad_activ)[0].astype(jnp.bfloat16)
    grad_w_in = jnp.dot(hidden_two.T, grad_pre, preferred_element_type=jnp.float32)
    grad_hidden_two = jnp.dot(grad_pre, full_in.T, preferred_element_type=jnp.float32).reshape(
        seqs, group, width
    )
    grad_shift_two, grad_scale_two, grad_gain_two, grad_normed_two = mod_back(
        grad_hidden_two, ln_two, normed_two, scale_two, vectors[1]
    )
    grad_mid = grad_y + norm_back(normed_two, inv_two, grad_normed_two)
    grad_gate_one = jnp.sum(grad_mid * branch_one, axis=1)
    grad_branch_one = (grad_mid * gate_one).astype(jnp.bfloat16).reshape(flat_rows, width)
    grad_w_attn = jnp.dot(attn_bf.T, grad_branch_one, preferred_element_type=jnp.float32)
    grad_attn_bf = (
        jnp.dot(grad_branch_one, full_attn.T, preferred_element_type=jnp.float32)
        .astype(jnp.bfloat16)
        .reshape(seqs, group, heads, HD)
    )
    delta = jnp.einsum("sqhd,shqd->shq", grad_attn_bf.astype(jnp.float32), attn_heads)
    kv_all = lax.all_gather(kv_local, "seq", axis=1, tiled=True)
    grad_queries = query_grads(kv_all, queries, grad_attn_bf, logsum, delta, width, factor)
    grad_kv = jnp.transpose(
        lax.psum_scatter(
            key_grads(
                kv_all,
                queries,
                grad_attn_bf,
                logsum,
                delta,
                width,
                factor,
                group * lax.axis_size("seq"),
            ).astype(jnp.bfloat16),
            "seq",
            scatter_dimension=0,
            tiled=True,
        ).astype(jnp.float32),
        (1, 0, 2),
    )
    grad_keys = grad_kv[..., :width].reshape(seqs, group, heads, HD)
    grad_qkv = jnp.concatenate(
        [
            rotate_back(grad_queries, cosines, sines).reshape(seqs, group, width),
            rotate_back(grad_keys, cosines, sines).reshape(seqs, group, width),
            grad_kv[..., width:],
        ],
        axis=-1,
    )
    grad_qkv = grad_qkv.astype(jnp.bfloat16).reshape(flat_rows, 3 * width)
    grad_w_qkv = jnp.dot(hidden_one.T, grad_qkv, preferred_element_type=jnp.float32)
    grad_hidden_one = jnp.dot(grad_qkv, full_qkv.T, preferred_element_type=jnp.float32).reshape(
        seqs, group, width
    )
    grad_shift_one, grad_scale_one, grad_gain_one, grad_normed_one = mod_back(
        grad_hidden_one, ln_one, normed_one, scale_one, vectors[0]
    )
    grad_start = grad_mid + norm_back(normed_one, inv_one, grad_normed_one)
    grad_mask_row = jnp.sum(jnp.where(masked[..., None], grad_start, 0.0), axis=(0, 1))
    grad_input = jnp.where(masked[..., None], 0.0, grad_start)
    grad_mod = jnp.concatenate(
        [
            grad_shift_one,
            grad_scale_one,
            grad_gate_one,
            grad_shift_two,
            grad_scale_two,
            grad_gate_two,
        ],
        axis=1,
    )
    grad_w_ada = jnp.dot(cond_bf.astype(jnp.float32).T, grad_mod, precision=lax.Precision.HIGHEST)
    grad_vectors = jnp.concatenate(
        [
            grad_gain_one[None, :],
            grad_gain_two[None, :],
            jnp.sum(grad_mod, axis=0).reshape(6, width),
            grad_mask_row[None, :],
        ],
        axis=0,
    )
    red_ada, red_qkv, red_attn, red_in, red_out, red_vec = (
        lax.psum_scatter(grad_w_ada, ("dp", "seq"), scatter_dimension=1, tiled=True),
        lax.psum_scatter(grad_w_qkv, ("dp", "seq"), scatter_dimension=0, tiled=True),
        lax.psum_scatter(grad_w_attn, ("dp", "seq"), scatter_dimension=0, tiled=True),
        lax.psum_scatter(grad_w_in, ("dp", "seq"), scatter_dimension=0, tiled=True),
        lax.psum_scatter(grad_w_out, ("dp", "seq"), scatter_dimension=0, tiled=True),
        lax.psum_scatter(grad_vectors, ("dp", "seq"), scatter_dimension=1, tiled=True),
    )
    local_squares = jnp.float32(0.0)
    for reduced in (red_vec, red_ada, red_qkv, red_attn, red_in, red_out):
        local_squares = local_squares + jnp.sum(reduced * reduced)
    grad_norm = jnp.sqrt(lax.psum(local_squares, ("dp", "seq")))
    clip_factor = jnp.minimum(1.0, CLIP / (grad_norm + 1e-06))
    columns = red_vec.shape[1]
    own_vectors = lax.dynamic_slice_in_dim(
        vectors, lax.axis_index(("dp", "seq")) * columns, columns, 1
    )
    vec_out = adam_step(own_vectors, red_vec * clip_factor, m_vec, v_vec, RATE_VECTORS, 0.0)
    ada_out = adam_step(w_ada, red_ada * clip_factor, m_ada, v_ada, RATE, DECAY)
    qkv_out = adam_step(w_qkv, red_qkv * clip_factor, m_qkv, v_qkv, RATE, DECAY)
    attn_out = adam_step(w_attn, red_attn * clip_factor, m_attn, v_attn, RATE, DECAY)
    in_out = adam_step(w_in, red_in * clip_factor, m_in, v_in, RATE, DECAY)
    out_out = adam_step(w_out, red_out * clip_factor, m_out, v_out, RATE, DECAY)
    return (
        block_out,
        grad_input,
        grad_norm,
        vec_out[0],
        vec_out[1],
        vec_out[2],
        ada_out[0],
        ada_out[1],
        ada_out[2],
        qkv_out[0],
        qkv_out[1],
        qkv_out[2],
        attn_out[0],
        attn_out[1],
        attn_out[2],
        in_out[0],
        in_out[1],
        in_out[2],
        out_out[0],
        out_out[1],
        out_out[2],
    )


F32, BF = jnp.float32, jnp.bfloat16
MESH = pl.DeviceIdType.MESH
DP, LINE, SEQ, CHIPS, ALL = 4, 4, 8, 16, 32
ROWS, WIDTH, PACK = 128, 768, 640
HALF = WIDTH // 2
HALVES = ((0, 0), (0, 1), (0, 2), (2, 2), (1, 0), (1, 1), (1, 2), None, (2, 0), (2, 1))

def numbered(**counts):
    at = {}
    for name, count in counts.items():
        at[name] = sum(counts[other] for other in at)
    return SimpleNamespace(**at), sum(counts.values())


S, SEM_COUNT = numbered(
    load=11,
    cond=1,
    mix_qkv=1,
    mix_in=1,
    mix_attn=1,
    mod=1,
    w_qkv=1,
    w_attn=4,
    plane_in=1,
    w_in=4,
    w_out=4,
    group_qkv=4,
    group_attn=4,
    fw_qkv=1,
    fw_attn=1,
    fw_in=1,
    fw_out=1,
    tok=4,
    h2=4,
    dm=4,
    xf=4,
    o=1,
    mm=1,
    dh2=1,
    do=1,
    gp=1,
    dh1=5,
    pair_out=1,
    pair_in=1,
    pair_attn=1,
    pair_qkv=1,
    plane_attn=1,
    plane_qkv=1,
    line_out=5,
    line_in=5,
    slice_in=1,
    line_attn=1,
    line_qkv=1,
    last_in=1,
    last_attn=1,
    last_qkv=1,
    early=7,
    late=7,
    sq=1,
)

SCRATCH = dict(
    i_tok=((1, 128, 768), BF),
    i_cot=((1, 128, 768), BF),
    i_vec=((9, 768), F32),
    i_wada=((144, 128), F32),
    i_wqkv=((24, 2304), F32),
    i_wattn=((24, 768), F32),
    i_win=((24, 3072), F32),
    i_wout=((96, 768), F32),
    wide_qkv=((48, 3072), F32),
    wide_in=((48, 3072), F32),
    wide_attn=((48, 768), F32),
    s_qkv=((48, 3072), BF),
    s_in=((48, 3072), BF),
    s_attn=((48, 768), BF),
    w_qkv=((768, 768), BF),
    w_in=((4, 4, 48, 768), BF),
    w_attn=((768, 768), BF),
    w_out=((4, 2, 96, 768), BF),
    t_w_qkv=((640, 768), BF),
    t_w_attn=((768, 1024), BF),
    t_w_in=((768, 768), BF),
    t_w_out=((768, 768), BF),
    t_h1=((768, 512), BF),
    conds_all=((4, 8, 128), F32),
    mod_send=((4, 4, 128), F32),
    mod_got=((32, 4, 128), F32),
    mod_flat=((40, 128), F32),
    mod_pad=((8, 384), F32),
    turn=((2, 4, 128, 128), F32),
    dmod_flat=((4, 40, 128), F32),
    mod=((8, 768), F32),
    x0=((128, 768), F32),
    n1=((4, 128, 768), F32),
    inv1=((4, 128, 128), F32),
    x1=((128, 768), F32),
    n2=((128, 768), F32),
    inv2=((128, 128), F32),
    a=((128, 768), F32),
    dx1=((128, 768), F32),
    toks=((4, 128, 768), BF),
    h1=((4, 128, 768), BF),
    h2=((4, 128, 768), BF),
    dm=((4, 128, 768), BF),
    gb=((4, 128, 768), BF),
    du=((4, 128, 768), BF),
    xb=((2, 4, 128, 640), BF),
    pt=((3, 1024, 512), BF),
    vt=((2, 128, 1024), BF),
    kt=((2, 128, 1024), BF),
    back=((4, 128, 768), F32),
    ot=((2, 128, 512), F32),
    os=((4, 192, 128), BF),
    ob=((4, 192, 128), BF),
    o2=((4, 128, 128), BF),
    mms=((4, 128, 768), BF),
    mmr=((4, 128, 768), BF),
    dhs=((4, 128, 768), BF),
    dhr=((4, 128, 768), BF),
    das=((128, 768), BF),
    dos=((4, 192, 128), BF),
    dob=((4, 192, 128), BF),
    dst=((3, 1024, 512), BF),
    ga=((512, 640), F32),
    gps=((512, 512), BF),
    gpr=((512, 512), BF),
    dqkv=((4, 128, 768), BF),
    d1s=((4, 128, 768), BF),
    d1r=((4, 128, 768), BF),
    g_out=((4, 2, 96, 768), BF),
    g_in=((2, 4, 4, 48, 384), BF),
    g_attn=((2, 768, 384), BF),
    g_qkv=((2, 768, 384), BF),
    p_out=((4, 96, 768), BF),
    p_in=((4, 4, 48, 384), BF),
    p_attn=((768, 384), BF),
    p_qkv=((768, 384), BF),
    q_attn=((4, 192, 384), BF),
    q_qkv=((4, 192, 384), BF),
    m_attn=((192, 384), BF),
    m_qkv=((192, 384), BF),
    r_out=((4, 96, 768), BF),
    r_in=((4, 4, 48, 384), BF),
    via_in=((4, 48, 384), BF),
    via_out=((96, 768), BF),
    via_dh1=((128, 768), BF),
    m_in=((4, 48, 384), BF),
    u_in=((4, 48, 384), BF),
    r_attn=((4, 48, 384), BF),
    r_qkv=((4, 48, 384), BF),
    t_in=((4, 48, 384), F32),
    t_attn=((1, 48, 384), F32),
    t_qkv=((4, 48, 384), F32),
    f_in=((4, 2, 24, 384), F32),
    f_attn=((1, 2, 24, 384), F32),
    f_qkv=((4, 2, 24, 384), F32),
    early=((8, 768), F32),
    early_pair=((8, 768), F32),
    early_line=((4, 8, 384), F32),
    early_plane=((4, 8, 384), F32),
    early_all=((2, 4, 8, 384), F32),
    late=((4, 768), F32),
    late_pair=((4, 768), F32),
    late_line=((4, 4, 384), F32),
    late_plane=((4, 4, 384), F32),
    late_all=((2, 4, 4, 384), F32),
    sq=((32, 1, 128), F32),
)


def dot(left, right):
    return jnp.dot(left, right, preferred_element_type=F32)


def dot_nt(left, right):
    return lax.dot_general(left, right, (((1,), (1,)), ((), ())), preferred_element_type=F32)


def dot_tn(left, right):
    return lax.dot_general(left, right, (((0,), (0,)), ((), ())), preferred_element_type=F32)


def loop(count, body, start=0):
    def step(index, carry):
        body(index)
        return carry

    lax.fori_loop(start, count, step, 0)


def layer_kernel(
    i_time,
    i_start,
    i_len,
    h_tok,
    h_cot,
    h_vec,
    h_wada,
    h_wqkv,
    h_wattn,
    h_win,
    h_wout,
    o_y,
    o_dx,
    o_norm,
    o_gqkv,
    o_gattn,
    o_gin,
    o_gout,
    o_dmod,
    o_gvec,
    o_vec,
    o_conds,
    *scratch,
):
    r = SimpleNamespace(**dict(zip(SCRATCH, scratch)), when=scratch[-3])
    send_sems, recv_sems = scratch[-2:]
    i_tok, i_cot, i_vec, i_wada = r.i_tok, r.i_cot, r.i_vec, r.i_wada
    i_wqkv, i_wattn, i_win, i_wout = r.i_wqkv, r.i_wattn, r.i_win, r.i_wout
    b, s = lax.axis_index("dp"), lax.axis_index("seq")
    z, c = lax.div(s, 2), lax.rem(s, 2)
    mate = s + 1 - 2 * c
    chip = b * LINE + z
    me = b * SEQ + s
    drains = []

    def push(src, dst, at, to_b, to_s, out=None):
        pltpu.make_async_remote_copy(
            src_ref=src,
            dst_ref=dst,
            send_sem=send_sems.at[at if out is None else out],
            recv_sem=recv_sems.at[at],
            device_id=(to_b, to_s),
            device_id_type=MESH,
        ).start()

    def keep(src, dst, at):
        pltpu.make_async_copy(src, dst, recv_sems.at[at]).start()

    def got(at, like):
        pltpu.make_async_copy(like, like, recv_sems.at[at]).wait()

    def left(at, like):
        pltpu.make_async_copy(like, like, send_sems.at[at]).wait()

    def sent(at, like):
        drains.append(lambda: left(at, like))

    def by_core(body):
        for h, width in ((0, HALF), (1, PACK - HALF)):

            @pl.when(c == h)
            def _():
                body(slice(HALF * h, HALF * h + width), width)

    def sent_by_core(at, like):
        drains.append(lambda: by_core(lambda columns, width: left(at, like(width))))

    near = (b, b + 1 - 2 * lax.rem(b, 2), b + 2 - 4 * lax.div(b, 2), 3 - b)

    def toward(k):
        if k == 3:
            return 3, near[3]
        slot = 1 + c if k == 1 else 2 - c
        return slot, (1 - c) * near[k] + c * near[3 - k]

    def peers(body):
        for k in (1, 2, 3):
            body(*toward(k))

    def stack(body):
        for k in (1, 2, 3):
            body(lax.rem(z + k + 2 * c * (2 - k), LINE))

    def line_gather(block, at, near=True, rest=True):
        inner = 1 + lax.rem(z, 2)
        if near:
            push(block(z), block(z), at + z, b, 2 * inner + c, at)

        def one(to):
            relayed = ((z == 1) & (to == 3)) | ((z == 2) & (to == 0))

            @pl.when(jnp.logical_not(relayed | (to == inner)))
            def _():
                push(block(z), block(z), at + z, b, 2 * to + c, at)

        if rest:
            stack(one)

    def line_relay(block, at):
        for middle, source, to in ((2, 1, 3), (1, 2, 0)):

            @pl.when(z == middle)
            def _():
                got(at + source, block(source))
                push(block(source), block(source), at + source, b, 2 * to + c, at)

    def line_got(block, at, k):
        here = (k == z) | ((z == 2) & (k == 1)) | ((z == 1) & (k == 2))

        @pl.when(jnp.logical_not(here))
        def _():
            got(at + k, block(0))

    far = lax.div(z, 2)

    def line_order(j):
        return lax.rem(z + (2, 3 - 2 * far, 1 + 2 * far, 0)[j], LINE)

    def line_add(j, rows, dst, via, at):
        to = line_order(j)
        outer_chip = (z == 0) | (z == 3)

        def direct():
            push(rows(to), dst.at[z], at + z, b, 2 * to + c, at)

        if j == 0:

            @pl.when(outer_chip)
            def _():
                push(rows(to), via, at + 4, b, 2 * (1 + far) + c, at)

            @pl.when(jnp.logical_not(outer_chip))
            def _():
                direct()

        elif j < 3:
            direct()
        else:
            keep(rows(z), dst.at[z], at + z)

    def line_via(via, at, add):
        @pl.when((z == 1) | (z == 2))
        def _():
            got(at + 4, via)
            add()

    def line_done(dst, at):
        for k in range(4):
            missing = ((z == 1) & (k == 3)) | ((z == 2) & (k == 0))

            @pl.when(jnp.logical_not(missing))
            def _():
                got(at + k, dst.at[k])

    def line_clear(dst):
        for middle, k in ((1, 3), (2, 0)):

            @pl.when(z == middle)
            def _():
                dst[k] = jnp.zeros(dst.shape[1:], BF)

    lane = lax.broadcasted_iota(jnp.int32, (1, 128), 1)
    low = lane < 64
    own24 = pl.ds(pl.multiple_of(24 * c, 8), 24)
    mate24 = pl.ds(pl.multiple_of(24 * (1 - c), 8), 24)
    part = pl.ds(pl.multiple_of(HALF * c, 128), HALF)
    chip_rows = pl.ds(pl.multiple_of(48 * chip, 16), 48)
    group_rows = pl.ds(pl.multiple_of(192 * b, 16), 192)

    barrier = pltpu.get_barrier_semaphore()

    def greet(k):
        other = lax.rem(me + k, ALL)
        pl.semaphore_signal(
            barrier, inc=1, device_id=(lax.div(other, SEQ), lax.rem(other, SEQ)), device_id_type=MESH
        )

    loads = (
        (i_time, r.when.at[0]),
        (i_start, r.when.at[1]),
        (i_len, r.when.at[2]),
        (h_wqkv, i_wqkv),
        (h_win, i_win),
        (h_wattn, i_wattn),
        (h_wout, i_wout),
        (h_tok, i_tok),
        (h_vec, i_vec),
        (h_wada, i_wada),
        (h_cot, i_cot),
    )
    for k, (src, dst) in enumerate(loads):
        pltpu.make_async_copy(src, dst, recv_sems.at[S.load + k]).start()
    loop(ALL, greet, 1)
    for k, (src, dst) in enumerate(loads):
        pltpu.make_async_copy(src, dst, recv_sems.at[S.load + k]).wait()

    def natural(kind, p, head):
        return kind * WIDTH + 192 * p + 64 * head

    def half_at(ref, column, high):
        tile = ref[:, column // 128 * 128 : column // 128 * 128 + 128]
        return tile if (column % 128 == 64) == high else pltpu.roll(tile, 64, 1)

    for p in range(4):
        for tile in range(5):
            pair = []
            for high in (0, 1):
                which = HALVES[2 * tile + high]
                pair.append(
                    jnp.zeros((24, 128), F32)
                    if which is None
                    else half_at(i_wqkv, natural(which[0], p, which[1]), bool(high))
                )
            r.wide_qkv[own24, 768 * p + 128 * tile : 768 * p + 128 * tile + 128] = jnp.where(
                low, pair[0], pair[1]
            )
        r.wide_qkv[own24, 768 * p + 640 : 768 * p + 768] = jnp.zeros((24, 128), F32)
    r.wide_in[own24, :] = i_win[...]
    r.wide_attn[own24, :] = i_wattn[...]
    r.w_out[z, c] = i_wout[...].astype(BF)
    r.toks[z] = i_tok[0]
    line_clear(r.r_out)
    line_clear(r.r_in)
    line_clear(r.d1r)
    for ref in (r.q_qkv, r.r_qkv):
        ref[:, :, PACK - HALF : HALF] = jnp.zeros((4, ref.shape[1], WIDTH - PACK), BF)
    lanes8 = lax.broadcasted_iota(jnp.int32, (8, 128), 1)
    half_cond = COND // 2
    speed = jnp.exp((lanes8 % half_cond).astype(F32) * (-math.log(10000.0) / half_cond))
    angle = r.when[0, 0].astype(F32) * speed
    wave = jnp.where(lanes8 < half_cond, jnp.cos(angle), jnp.sin(angle))
    r.conds_all[b] = wave * (1.0 / (1.0 + jnp.exp(-wave)))
    pl.semaphore_wait(barrier, ALL - 1)

    def token_block(k):
        return r.toks.at[k]

    def attn_block(k):
        return r.w_attn.at[pl.ds(pl.multiple_of(192 * b + 48 * k, 16), 48), part]

    def in_block(k):
        return r.w_in.at[:, k, :, part]

    def out_block(k):
        return r.w_out.at[k, c]

    peers(lambda k, to: push(r.conds_all.at[b], r.conds_all.at[b], S.cond, to, s))
    sent(S.cond, r.conds_all.at[0:3])
    push(r.wide_qkv.at[own24], r.wide_qkv.at[own24], S.mix_qkv, b, mate)
    sent(S.mix_qkv, r.wide_qkv.at[0:24])
    push(r.wide_attn.at[own24], r.wide_attn.at[own24], S.mix_attn, b, mate)
    sent(S.mix_attn, r.wide_attn.at[0:24])
    push(r.wide_in.at[own24], r.wide_in.at[own24], S.mix_in, b, mate)
    sent(S.mix_in, r.wide_in.at[0:24])

    got(S.cond, r.conds_all.at[0:3])
    row8 = lax.broadcasted_iota(jnp.int32, (8, 128), 0)
    cond4 = jnp.zeros((8, 128), F32)
    for k in range(4):
        cond4 = jnp.where(row8 == k, r.conds_all[k], cond4)
    o_conds[...] = cond4
    wide = i_wada.shape[0]
    r.mod_pad[...] = jnp.zeros((8, 384), F32)
    r.mod_pad[:, 0:wide] = dot_nt(cond4.astype(BF), i_wada[...].astype(BF))
    columns = pltpu.roll(r.mod_pad[...], lax.rem(wide * me, 128), 1)
    for k in range(4):
        for t in range(3):
            r.mod_send[k, t : t + 1, :] = columns[k : k + 1, 128 * t : 128 * t + 128]
        r.mod_send[k, 3:4, :] = jnp.zeros((1, 128), F32)

    def send_mod(k):
        other = lax.rem(me + k, ALL)
        ob = lax.div(other, SEQ)
        push(r.mod_send.at[ob], r.mod_got.at[me], S.mod, ob, lax.rem(other, SEQ))

    loop(ALL, send_mod, 1)
    sent(S.mod, r.mod_got.at[0:31])
    keep(r.mod_send.at[b], r.mod_got.at[me], S.mod)

    def block(src, first):
        return src.at[:, pl.ds(pl.multiple_of(first, 128), HALF)]

    def slices_along_line():
        def send(columns, width):
            def rows(to):
                first = pl.multiple_of(WIDTH * to + columns.start, 128)
                return r.s_qkv.at[:, pl.ds(first, width)]

            dst = r.w_qkv.at[chip_rows, columns]
            stack(lambda to: push(rows(to), dst, S.w_qkv, b, 2 * to + c))
            keep(rows(z), dst, S.w_qkv)

        by_core(send)
        sent_by_core(S.w_qkv, lambda width: r.w_qkv.at[0:144, 0:width])

    def over_plane(dst, at):
        rows = dst.at[group_rows, part]
        peers(lambda k, to: push(rows, rows, at + k, to, s))
        for k in (1, 2, 3):
            sent(at + k, dst.at[0:192, 0:HALF])

    def share(dst, at, onward):
        for k in range(4):
            rows = dst.at[pl.ds(pl.multiple_of(192 * near[k], 16), 192), part]
            if k:
                got(at + k, rows)
            push(rows, rows, onward, b, mate)
        sent(onward, dst.at[:, 0:HALF])

    def line_share(block, at, onward):
        for k in range(4):
            line_got(block, at, k)
            push(block(k), block(k), onward, b, mate)

    got(S.mix_qkv, r.wide_qkv.at[0:24])
    r.s_qkv[...] = r.wide_qkv[...].astype(BF)
    slices_along_line()
    line_gather(token_block, S.tok, rest=False)
    sent(S.tok, r.toks.at[0:3])
    got(S.mix_attn, r.wide_attn.at[0:24])
    r.s_attn[...] = r.wide_attn[...].astype(BF)

    def qkv_over_plane(columns, width):
        got(S.w_qkv, r.w_qkv.at[0:192, 0:width])
        rows = r.w_qkv.at[group_rows, columns]
        peers(lambda k, to: push(rows, rows, S.group_qkv + k, to, s))

    by_core(qkv_over_plane)
    for k in (1, 2, 3):
        sent_by_core(S.group_qkv + k, lambda width: r.w_qkv.at[0:192, 0:width])
    line_gather(token_block, S.tok, near=False)
    for h in range(2):

        @pl.when(c == h)
        def _():
            r.w_attn[chip_rows, 384 * h : 384 * h + 384] = r.s_attn[:, 384 * h : 384 * h + 384]

    line_gather(attn_block, S.w_attn)
    sent(S.w_attn, r.w_attn.at[0:144, 0:HALF])
    line_gather(out_block, S.w_out)
    sent(S.w_out, r.w_out.at[0:3, 0])
    got(S.mix_in, r.wide_in.at[0:24])
    r.s_in[...] = r.wide_in[...].astype(BF)
    peers(
        lambda k, to: push(
            block(r.s_in, WIDTH * to + HALF * c), r.w_in.at[b, z, :, part], S.plane_in, to, s
        )
    )
    keep(block(r.s_in, WIDTH * b + HALF * c), r.w_in.at[b, z, :, part], S.plane_in)
    sent(S.plane_in, r.w_in.at[0:3, 0, :, 0:HALF])

    def hidden_rows(k):
        place = (2 * k + c) * ROWS + lax.broadcasted_iota(jnp.int32, (ROWS, 1), 0)
        return (place >= r.when[1, 0]) & (place < r.when[1, 0] + r.when[2, 0])

    def first_norm(tokens, k):
        x0 = jnp.where(hidden_rows(k), i_vec[8:9, :], tokens.astype(F32))
        normed, inverse = normalize(x0)
        r.n1[k] = normed
        r.inv1[k] = jnp.broadcast_to(inverse, (ROWS, 128))
        return x0

    r.x0[...] = first_norm(i_tok[0], z)

    got(S.mod, r.mod_got)
    r.mod_flat[...] = jnp.zeros((40, 128), F32)
    for k in range(ALL):
        first = 9 * k // 8
        r.mod_flat[first : first + 3, :] += r.mod_got[k, 0:3, :]
    for k in range(6):
        row = jnp.concatenate(
            [r.mod_flat[6 * k + t : 6 * k + t + 1, :] for t in range(6)], axis=1
        )
        r.mod[k : k + 1, :] = row + i_vec[2 + k : 3 + k, :]

    def mod(k):
        return r.mod[k : k + 1, :]

    def vec(k):
        return i_vec[k : k + 1, :]

    r.h1[z] = (r.n1[z] * vec(0) * (1.0 + mod(1)) + mod(0)).astype(BF)
    r.dm[0] = (i_cot[0].astype(F32) * mod(5)).astype(BF)
    peers(lambda k, to: push(r.dm.at[0], r.dm.at[k], S.dm + k, to, s))
    for k in (1, 2, 3):
        sent(S.dm + k, r.dm.at[0])

    lanes = lax.broadcasted_iota(jnp.int32, (ROWS, 128), 1)
    first_half = lanes % HD < HD // 2
    speed = jnp.exp((lanes % (HD // 2)).astype(F32) * (-math.log(10000.0) / (HD // 2)))
    row = lax.broadcasted_iota(jnp.int32, (ROWS, 128), 0)

    def table(k):
        angle = ((2 * k + c) * ROWS + row).astype(F32) * speed
        r.turn[0, k] = jnp.cos(angle)
        sine = jnp.sin(angle)
        r.turn[1, k] = jnp.where(first_half, -sine, sine)

    loop(LINE, table)

    line_relay(token_block, S.tok)

    def qkv_share(columns, width):
        for k in range(4):
            rows = r.w_qkv.at[pl.ds(pl.multiple_of(192 * near[k], 16), 192), columns]
            if k:
                got(S.group_qkv + k, rows)
            push(rows, rows, S.fw_qkv, b, mate)

    by_core(qkv_share)
    sent_by_core(S.fw_qkv, lambda width: r.w_qkv.at[:, 0:width])
    by_core(lambda columns, width: got(S.fw_qkv, r.w_qkv.at[:, 0 : PACK - width]))
    for k in range(5):
        columns = slice(128 * k, 128 * k + 128)
        r.t_w_qkv[columns, :] = r.w_qkv[:, columns].T

    def turned(tile, sign, k):
        other = jnp.where(first_half, pltpu.roll(tile, 96, 1), pltpu.roll(tile, 32, 1))
        return tile * r.turn[0, k] + sign * (other * r.turn[1, k])

    def project(j):
        k = lax.rem(z + j, LINE)

        @pl.when(j > 0)
        def _():
            line_got(token_block, S.tok, k)
            first_norm(r.toks[k], k)
            r.h1[k] = (r.n1[k] * vec(0) * (1.0 + mod(1)) + mod(0)).astype(BF)

        x = dot(r.h1[k], r.w_qkv[:, 0:PACK])
        tiles = [x[:, 128 * t : 128 * t + 128] for t in range(5)]
        tiles[0] = turned(tiles[0], 1.0, k) * 0.125
        tiles[1] = jnp.where(low, turned(tiles[1], 1.0, k) * 0.125, tiles[1])
        tiles[2] = turned(tiles[2], 1.0, k)
        tiles[3] = turned(tiles[3], 1.0, k)
        for t in range(5):
            r.xb[0, k, :, 128 * t : 128 * t + 128] = tiles[t].astype(BF)
        push(r.xb.at[0, k], r.xb.at[1, k], S.xf + k, b, mate)

    loop(4, project)
    line_relay(attn_block, S.w_attn)
    for k in range(4):
        line_got(attn_block, S.w_attn, k)
    over_plane(r.w_attn, S.group_attn)
    for k in range(4):
        sent(S.xf + k, r.xb.at[0, 0])

    for k in range(6):
        columns = slice(128 * k, 128 * k + 128)
        r.t_h1[columns, :] = r.h1[:, :, columns].reshape(512, 128).T
    for k in range(4):
        got(S.xf + k, r.xb.at[0, 0])

    def tile_of(t):
        return r.xb[:, :, :, 128 * t : 128 * t + 128].reshape(1024, 128)

    heads = ((0, 2, 4, True, True), (0, 2, 4, False, False), (1, 3, 1, True, False))

    def queries(head, first, size):
        q_tile, _, _, q_low, _ = heads[head]
        q = r.xb[0, first : first + size, :, 128 * q_tile : 128 * q_tile + 128]
        return jnp.where(low if q_low else ~low, q.reshape(size * 128, 128), jnp.zeros((), BF))

    r.vt[0] = tile_of(4).T
    r.vt[1] = tile_of(1).T
    for half in range(2):
        at = slice(256 * half, 256 * half + 256)
        for head in range(3):
            scores = dot_nt(tile_of(heads[head][1]), queries(head, 2 * half, 2))
            weights = jnp.exp(scores - jnp.max(scores, axis=0, keepdims=True))
            weights = weights * (1.0 / jnp.sum(weights, axis=0, keepdims=True))
            weights = weights.astype(BF)
            r.pt[head, :, at] = weights
            out = dot(r.vt[head // 2], weights)
            if head == 0:
                r.ot[0, 0:64, at] = out[0:64]
            elif head == 1:
                r.ot[0, 64:128, at] = out[64:128]
            else:
                r.ot[1, 0:64, at] = out[64:128]
                r.ot[1, 64:128, at] = jnp.zeros((64, 256), F32)
        for k in (2 * half, 2 * half + 1):
            across = slice(128 * k, 128 * k + 128)
            r.os[k, 0:128, :] = r.ot[0, :, across].T.astype(BF)
            third = r.ot[1, 0:64, across]
            third = jnp.concatenate([third, pltpu.roll(third, 64, 1)], axis=0)
            r.os[k, 128:192, :] = third.T[0:64].astype(BF)
        for to in (2 * half, 2 * half + 1):

            @pl.when(z == to)
            def _():
                keep(r.os.at[to], r.ob.at[z], S.o)

            @pl.when(z != to)
            def _():
                push(r.os.at[to], r.ob.at[z], S.o, b, 2 * to + c)

        if half == 0:
            line_relay(out_block, S.w_out)

    sent(S.o, r.os.at[0:3])
    got(S.plane_in, r.w_in.at[:, 0, :, 0:HALF])
    line_gather(in_block, S.w_in)
    sent(S.w_in, r.w_in.at[0:3, :, :, 0:HALF])
    for k in range(2):
        r.kt[k] = tile_of(2 + k).T
    share(r.w_attn, S.group_attn, S.fw_attn)
    got(S.fw_attn, r.w_attn.at[:, 0:HALF])
    for p in range(4):
        first = 192 * p
        r.t_w_attn[:, 256 * p : 256 * p + 128] = r.w_attn[first : first + 128, :].T
        third = r.w_attn[first + 128 : first + 192, :]
        r.t_w_attn[:, 256 * p + 128 : 256 * p + 256] = jnp.concatenate(
            [third, jnp.zeros_like(third)], axis=0
        ).T
    got(S.o, r.ob)
    a = jnp.zeros((ROWS, WIDTH), F32)
    for p in range(4):
        third = r.ob[p, 128:192, :].astype(F32)
        third = jnp.concatenate([third, pltpu.roll(third, 64, 1)], axis=0)
        r.o2[p] = jnp.where(low, third, 0.0).astype(BF)
        a += dot(r.ob[p, 0:128, :], r.w_attn[192 * p : 192 * p + 128, :])
        a += dot(r.o2[p, :, 0:64], r.w_attn[192 * p + 128 : 192 * p + 192, :])
    r.a[...] = a
    x1 = r.x0[...] + mod(2) * a
    r.x1[...] = x1
    n2, inv2 = normalize(x1)
    r.n2[...] = n2
    r.inv2[...] = jnp.broadcast_to(inv2, (ROWS, 128))
    r.h2[0] = (n2 * vec(1) * (1.0 + mod(4)) + mod(3)).astype(BF)
    peers(lambda k, to: push(r.h2.at[0], r.h2.at[k], S.h2 + k, to, s))
    for k in (1, 2, 3):
        sent(S.h2 + k, r.h2.at[0])
    line_relay(in_block, S.w_in)
    line_share(out_block, S.w_out, S.fw_out)
    sent(S.fw_out, r.w_out.at[:, 0])
    got(S.fw_out, r.w_out.at[:, 0])

    for k in range(6):
        columns = slice(128 * k, 128 * k + 128)
        r.t_w_out[columns, :] = r.w_out[:, :, :, columns].reshape(WIDTH, 128).T

    def feed_back(k):
        @pl.when(k > 0)
        def _():
            got(S.dm + k, r.dm.at[0])

        r.back[k] = dot(r.dm[k], r.t_w_out[...])

    loop(4, feed_back)
    line_share(in_block, S.w_in, S.fw_in)
    sent(S.fw_in, r.w_in.at[:, :, :, 0:HALF])
    got(S.fw_in, r.w_in.at[:, :, :, 0:HALF])
    for k in range(6):
        columns = slice(128 * k, 128 * k + 128)
        r.t_w_in[columns, :] = r.w_in[:, :, :, columns].reshape(WIDTH, 128).T

    def feed(first, count):
        at = slice(first, first + count)
        size = count * ROWS
        u = dot(r.h2[at].reshape(size, WIDTH), r.w_in[...].reshape(WIDTH, WIDTH))
        slope = 0.7978845608028654
        cube = 0.044715
        t = jnp.tanh(slope * (u + cube * u * u * u))
        r.gb[at] = (0.5 * u * (1.0 + t)).astype(BF).reshape(count, ROWS, WIDTH)
        bend = 0.5 * (1.0 + t) + 0.5 * u * (1.0 - t * t) * (slope * (1.0 + 3.0 * cube * u * u))
        du = (r.back[at].reshape(size, WIDTH) * bend).astype(BF)
        r.du[at] = du.reshape(count, ROWS, WIDTH)
        r.dhs[at] = dot(du, r.t_w_in[...]).astype(BF).reshape(count, ROWS, WIDTH)

    feed(0, 1)
    for first, count in ((1, 2), (3, 1)):
        for k in range(first, first + count):
            got(S.h2 + k, r.h2.at[0])
        feed(first, count)
        for k in range(first, first + count):
            slot, to = toward(k)
            push(r.dhs.at[slot], r.dhr.at[slot], S.dh2, to, s)
    sent(S.dh2, r.dhs.at[0:3])
    def gather(own, others):
        total = own[0].astype(F32)
        for k in (1, 2, 3):
            total += others[k].astype(F32)
        return total

    for k in range(2):
        rows = slice(384 * k, 384 * k + 384)
        result = dot_tn(r.gb[:, :, rows].reshape(512, 384), r.dm[...].reshape(512, 768))
        r.g_out[2 * k : 2 * k + 2] = result.astype(BF).reshape(2, 2, 96, 768)
    push(r.g_out.at[:, 1 - c], r.p_out, S.pair_out, b, mate)
    sent(S.pair_out, r.p_out)

    def to_mate(grad, dst, at):
        push(grad.at[1 - c], dst, at, b, mate)
        sent(at, dst)

    def pair_sum(grad, pair, at):
        got(at, pair)
        grad[c] = (grad[c].astype(F32) + pair[...].astype(F32)).astype(BF)

    def plane_sum(grad, dst, at, packed=False):
        def send(columns, width):
            def rows(to):
                return grad.at[c, pl.ds(pl.multiple_of(192 * to, 16), 192), 0:width]

            peers(lambda k, to: push(rows(to), dst.at[k, :, 0:width], at, to, s))
            keep(rows(b), dst.at[0, :, 0:width], at)

        if packed:
            by_core(send)
            sent_by_core(at, lambda width: dst.at[0:3, :, 0:width])
        else:
            send(None, HALF)
            sent(at, dst.at[0:3])

    def line_sum(src, total, dst, first, at, packed=False):
        def send(columns, width):
            got(first, src.at[:, :, 0:width])
            total[...] = (
                (src[0].astype(F32) + src[1].astype(F32))
                + (src[2].astype(F32) + src[3].astype(F32))
            ).astype(BF)

            def rows(to):
                return total.at[pl.ds(pl.multiple_of(48 * to, 16), 48), 0:width]

            stack(lambda to: push(rows(to), dst.at[z, :, 0:width], at, b, 2 * to + c))
            keep(rows(z), dst.at[z, :, 0:width], at)

        if packed:
            by_core(send)
            sent_by_core(at, lambda width: dst.at[0:3, :, 0:width])
        else:
            send(None, HALF)
            sent(at, dst.at[0:3])

    def trade(total, final, at):
        push(total.at[:, mate24], final.at[:, c], at, b, mate)
        sent(at, final.at[:, 0])
        final[:, c] = total[:, own24, :]

    def in_product(k):
        rows = slice(384 * k, 384 * k + 384)
        result = dot_tn(r.h2[:, :, rows].reshape(512, 384), r.du[...].reshape(512, 768)).astype(BF)
        for h in range(2):
            r.g_in[h, 2 * k : 2 * k + 2] = result[:, 384 * h : 384 * h + 384].reshape(2, 4, 48, 384)

    in_product(0)

    got(S.pair_out, r.p_out)
    for k in range(4):
        r.g_out[k, c] = (r.g_out[k, c].astype(F32) + r.p_out[k].astype(F32)).astype(BF)

    def out_rows(k):
        return r.g_out.at[k, c]

    for j in (0, 1):
        line_add(j, out_rows, r.r_out, r.via_out, S.line_out)
    in_product(1)
    to_mate(r.g_in, r.p_in, S.pair_in)

    def add_out():
        k = line_order(2)
        r.g_out[k, c] = (r.g_out[k, c].astype(F32) + r.via_out[...].astype(F32)).astype(BF)

    got(S.dh2, r.dhr.at[0:3])
    dh = gather(r.dhs, r.dhr)
    n2 = r.n2[...]
    inv2 = r.inv2[:, 0:1]
    r.early[...] = jnp.zeros((8, 768), F32)
    r.early[2:3, :] = jnp.sum(dh, axis=0, keepdims=True)
    both = jnp.sum(dh * n2, axis=0, keepdims=True)
    r.early[3:4, :] = both * vec(1)
    r.early[0:1, :] = both * (1.0 + mod(4))
    grad = dh * ((1.0 + mod(4)) * vec(1))
    dx1 = i_cot[0].astype(F32) + norm_back(n2, inv2, grad)
    r.dx1[...] = dx1
    r.early[1:2, :] = jnp.sum(dx1 * r.a[...], axis=0, keepdims=True)
    r.das[...] = (dx1 * mod(2)).astype(BF)
    for p in range(4):
        result = dot(r.das[...], r.t_w_attn[:, 256 * p : 256 * p + 256])
        r.dos[p, 0:128, :] = result[:, 0:128].astype(BF)
        third = result[:, 128:256]
        third = jnp.where(low, third[0:64], pltpu.roll(third[64:128], 64, 1))
        r.dos[p, 128:192, :] = third.astype(BF)
    stack(lambda to: push(r.dos.at[to], r.dob.at[z], S.do, b, 2 * to + c))
    keep(r.dos.at[z], r.dob.at[z], S.do)
    sent(S.do, r.dos.at[0:3])
    for t in range(3):
        at = slice(256 * t, 256 * t + 256)
        mm = dot(r.gb[...].reshape(512, WIDTH), r.w_out[:, :, :, at].reshape(WIDTH, 256))
        r.mms[:, :, at] = mm.astype(BF).reshape(4, ROWS, 256)
    peers(lambda k, to: push(r.mms.at[k], r.mmr.at[k], S.mm, to, s))
    sent(S.mm, r.mms.at[0:3])

    for p in range(4):
        for rows, left_side in (
            (slice(192 * p, 192 * p + 128), r.ob[p, 0:128, :]),
            (slice(192 * p + 128, 192 * p + 192), r.o2[p]),
        ):
            result = dot_tn(left_side, r.das[...])[0 : rows.stop - rows.start].astype(BF)
            r.g_attn[0, rows, :] = result[:, 0:HALF]
            r.g_attn[1, rows, :] = result[:, HALF:WIDTH]
    to_mate(r.g_attn, r.p_attn, S.pair_attn)

    def small_sum(src, pair, line, plane, whole, at):
        def first():
            push(src, pair, at, b, mate)
            sent(at, src)

        def second():
            got(at, pair)
            total = src[...] + pair[...]
            line[z] = (1 - c) * total[:, 0:HALF] + c * total[:, HALF:WIDTH]
            stack(lambda to: push(line.at[z], line.at[z], at + 1, b, 2 * to + c))
            sent(at + 1, line.at[0:3])

        def third():
            got(at + 1, line.at[0:3])
            plane[b] = (line[0] + line[1]) + (line[2] + line[3])
            peers(lambda k, to: push(plane.at[b], plane.at[b], at + 2, to, s))
            sent(at + 2, plane.at[0:3])

        def fourth():
            got(at + 2, plane.at[0:3])
            whole[c] = plane[...]
            push(plane, whole.at[c], at + 3, b, mate)
            sent(at + 3, plane)

        def rows(k):
            return jnp.concatenate([whole[0, k], whole[1, k]], axis=1)

        return first, second, third, fourth, rows

    early_steps = small_sum(
        r.early, r.early_pair, r.early_line, r.early_plane, r.early_all, S.early
    )
    late_steps = small_sum(r.late, r.late_pair, r.late_line, r.late_plane, r.late_all, S.late)

    pair_sum(r.g_in, r.p_in, S.pair_in)
    line_via(r.via_out, S.line_out, add_out)
    for j in (2, 3):
        line_add(j, out_rows, r.r_out, r.via_out, S.line_out)
    sent(S.line_out, r.r_out.at[0:3])

    def in_rows(k):
        return r.g_in.at[c, :, k]

    for j in (0, 1):
        line_add(j, in_rows, r.r_in, r.via_in, S.line_in)

    def add_in():
        k = line_order(2)
        r.g_in[c, :, k] = (r.g_in[c, :, k].astype(F32) + r.via_in[...].astype(F32)).astype(BF)

    pair_sum(r.g_attn, r.p_attn, S.pair_attn)
    plane_sum(r.g_attn, r.q_attn, S.plane_attn)

    got(S.do, r.dob)
    dot0 = r.dob[:, 0:128, :].reshape(512, 128)
    third = r.dob[:, 128:192, :].astype(F32).reshape(256, 128)
    other_rows = jnp.where(low, pltpu.roll(third, 64, 1), 0.0).reshape(4, 64, 128)
    third = jnp.where(low, third, 0.0).reshape(4, 64, 128)
    dot1 = jnp.concatenate([third, other_rows], axis=1).reshape(512, 128)
    zero = jnp.zeros((), BF)
    moved = pltpu.roll(dot1, 64, 1).astype(BF)
    grads = (jnp.where(low, dot0, zero), jnp.where(low, zero, dot0), moved)
    product = dot0.astype(F32).T * r.ot[0]
    deltas = (
        jnp.sum(product[0:64], axis=0, keepdims=True),
        jnp.sum(product[64:128], axis=0, keepdims=True),
        jnp.sum(dot1.T * r.ot[1], axis=0, keepdims=True),
    )
    for head in range(3):
        values = tile_of(heads[head][2])
        for half in range(2):
            at = slice(256 * half, 256 * half + 256)
            dp = dot_nt(values, grads[head][at])
            r.dst[head, :, at] = (
                r.pt[head, :, at].astype(F32) * (dp - deltas[head][:, at])
            ).astype(BF)

    def key_grads(rows):
        dk = [dot(r.dst[head, rows, :], queries(head, 0, 4)) for head in range(3)]
        dv = [dot(r.pt[head, rows, :], grads[head]) for head in range(3)]
        return (dv[2], dk[0] + dk[1], dk[2], dv[0] + dv[1])

    for t, tile in enumerate(key_grads(slice(512, 1024))):
        r.gps[:, 128 * t : 128 * t + 128] = tile.astype(BF)
    push(r.gps, r.gpr, S.gp, b, mate)
    sent(S.gp, r.gps)
    for t, tile in enumerate(key_grads(slice(0, 512))):
        r.ga[:, 128 * t + 128 : 128 * t + 256] = tile
    for half in range(2):
        at = slice(256 * half, 256 * half + 256)
        turned_q = [dot(r.kt[head // 2], r.dst[head, :, at]) for head in range(3)]
        top = jnp.concatenate([turned_q[0][0:64], turned_q[1][64:128]], axis=0)
        r.ga[at, 0:128] = top.T * 0.125
        r.ga[at, 128:256] += turned_q[2].T * 0.125
    line_via(r.via_in, S.line_in, add_in)
    for j in (2, 3):
        line_add(j, in_rows, r.r_in, r.via_in, S.line_in)
    sent(S.line_in, r.r_in.at[0:3])
    got(S.gp, r.gpr)

    def dh1_rows(k):
        return r.d1s.at[k]

    def back_turn(k):
        rows = pl.ds(pl.multiple_of(128 * k, 128), 128)
        tiles = [r.ga[rows, 0:128]] + [
            r.ga[rows, 128 * t : 128 * t + 128]
            + r.gpr[rows, 128 * t - 128 : 128 * t].astype(F32)
            for t in range(1, 5)
        ]
        tiles[0] = turned(tiles[0], -1.0, k)
        tiles[1] = jnp.where(low, turned(tiles[1], -1.0, k), tiles[1])
        tiles[2] = turned(tiles[2], -1.0, k)
        tiles[3] = turned(tiles[3], -1.0, k)
        for t in range(5):
            r.dqkv[k, :, 128 * t : 128 * t + 128] = tiles[t].astype(BF)
        r.dqkv[k, :, PACK:WIDTH] = jnp.zeros((128, 128), BF)

    back_turn(line_order(0))

    def unproject(j):
        k = line_order(j)
        partial_sum = dot(r.dqkv[k, :, 0:PACK], r.t_w_qkv[...])
        r.d1s[k] = partial_sum.astype(BF)
        if j == 2:

            def add():
                r.d1s[k] = (partial_sum + r.via_dh1[...].astype(F32)).astype(BF)

            line_via(r.via_dh1, S.dh1, add)
        line_add(j, dh1_rows, r.d1r, r.via_dh1, S.dh1)
        n = r.n1[k]
        e = partial_sum * ((1.0 + mod(1)) * vec(0))
        weight = jnp.where(hidden_rows(k), r.inv1[k][:, 0:1], 0.0)
        centred = (
            e
            - jnp.mean(e, axis=-1, keepdims=True)
            - n * jnp.mean(e * n, axis=-1, keepdims=True)
        )
        r.late[0:1, :] += jnp.sum(partial_sum * n, axis=0, keepdims=True)
        r.late[1:2, :] += jnp.sum(partial_sum, axis=0, keepdims=True)
        r.late[3:4, :] += jnp.sum(weight * centred, axis=0, keepdims=True)

    r.late[...] = jnp.zeros((4, 768), F32)
    r.late[3:4, :] = jnp.sum(
        jnp.where(hidden_rows(z), r.dx1[...], 0.0), axis=0, keepdims=True
    )
    unproject(0)
    for j in (1, 2, 3):
        back_turn(line_order(j))

    def qkv_rows(k):
        rows = pl.ds(pl.multiple_of(128 * k, 128), 128)
        result = dot(r.t_h1[rows, :], r.dqkv[...].reshape(512, WIDTH)).astype(BF)
        r.g_qkv[0, rows, :] = result[:, 0:HALF]
        r.g_qkv[1, rows, :] = result[:, HALF:WIDTH]

    loop(6, qkv_rows)
    to_mate(r.g_qkv, r.p_qkv, S.pair_qkv)
    unproject(1)
    pair_sum(r.g_qkv, r.p_qkv, S.pair_qkv)
    plane_sum(r.g_qkv, r.q_qkv, S.plane_qkv, True)
    got(S.mm, r.mmr.at[0:3])
    mm = gather(r.mms, r.mmr)
    o_y[...] = (r.x1[...] + mod(5) * mm).astype(BF)
    r.early[4:5, :] = jnp.sum(i_cot[0].astype(F32) * mm, axis=0, keepdims=True)
    early_steps[0]()
    unproject(2)
    unproject(3)
    sent(S.dh1, r.d1s.at[0:3])
    both = r.late[0:1, :]
    r.late[2:3, :] = both * vec(0)
    r.late[0:1, :] = both * (1.0 + mod(1))
    late_steps[0]()
    early_steps[1]()
    line_sum(r.q_attn, r.m_attn, r.r_attn, S.plane_attn, S.line_attn)
    late_steps[1]()

    line_done(r.r_in, S.line_in)
    r.m_in[...] = (
        (r.r_in[0].astype(F32) + r.r_in[1].astype(F32))
        + (r.r_in[2].astype(F32) + r.r_in[3].astype(F32))
    ).astype(BF)
    peers(lambda k, to: push(r.m_in.at[to], r.u_in.at[b], S.slice_in, to, s))
    keep(r.m_in.at[b], r.u_in.at[b], S.slice_in)
    sent(S.slice_in, r.u_in.at[0:3])
    line_sum(r.q_qkv, r.m_qkv, r.r_qkv, S.plane_qkv, S.line_qkv, True)
    early_steps[2]()
    late_steps[2]()

    line_done(r.d1r, S.dh1)
    dh = (r.d1r[0].astype(F32) + r.d1r[1].astype(F32)) + (
        r.d1r[2].astype(F32) + r.d1r[3].astype(F32)
    )
    n1 = r.n1[z]
    grad = dh * ((1.0 + mod(1)) * vec(0))
    dx0 = r.dx1[...] + norm_back(n1, r.inv1[z][:, 0:1], grad)
    o_dx[...] = jnp.where(hidden_rows(z), 0.0, dx0)
    early_steps[3]()
    late_steps[3]()

    line_done(r.r_out, S.line_out)
    total = (r.r_out[0].astype(F32) + r.r_out[1].astype(F32)) + (
        r.r_out[2].astype(F32) + r.r_out[3].astype(F32)
    )
    o_gout[...] = total
    squares = total * total
    squares = jnp.sum(squares[:, 0:128] + squares[:, 128:256] + squares[:, 256:384]
                      + squares[:, 384:512] + squares[:, 512:640] + squares[:, 640:768],
                      axis=0, keepdims=True)

    def fold(value):
        total = value[:, 0:128] * value[:, 0:128]
        for t in range(1, value.shape[1] // 128):
            total += value[:, 128 * t : 128 * t + 128] * value[:, 128 * t : 128 * t + 128]
        return jnp.sum(total, axis=0, keepdims=True)

    got(S.slice_in, r.u_in)
    r.t_in[...] = r.u_in[...].astype(F32)
    for p in range(4):
        squares += fold(r.t_in[p])
    trade(r.t_in, r.f_in, S.last_in)
    got(S.line_attn, r.r_attn)
    r.t_attn[0] = (r.r_attn[0].astype(F32) + r.r_attn[1].astype(F32)) + (
        r.r_attn[2].astype(F32) + r.r_attn[3].astype(F32)
    )
    squares += fold(r.t_attn[0])
    trade(r.t_attn, r.f_attn, S.last_attn)
    by_core(lambda columns, width: got(S.line_qkv, r.r_qkv.at[:, :, 0:width]))
    r.t_qkv[...] = r.r_qkv[...].astype(F32)
    trade(r.t_qkv, r.f_qkv, S.last_qkv)
    for p in range(4):
        squares += fold(r.t_qkv[p])
    r.sq[me] = squares

    def send_sq(k):
        other = lax.rem(me + k, ALL)
        push(r.sq.at[me], r.sq.at[me], S.sq, lax.div(other, SEQ), lax.rem(other, SEQ))

    loop(ALL, send_sq, 1)
    sent(S.sq, r.sq.at[0:31])
    got(S.last_in, r.f_in.at[:, 0])
    got(S.last_attn, r.f_attn.at[:, 0])
    for h in range(2):
        for p in range(4):
            value = r.f_in[p, h]
            o_gin[:, 768 * p + 384 * h : 768 * p + 384 * h + 384] = value
        value = r.f_attn[0, h]
        o_gattn[:, 384 * h : 384 * h + 384] = value
    got(S.last_qkv, r.f_qkv.at[:, 0])
    where = {which: index for index, which in enumerate(HALVES) if which is not None}

    def packed_half(chunk, high):
        kind, rest = chunk // 12, chunk % 12
        index = where[(kind, rest % 3)]
        t = index // 2
        tile = r.f_qkv[rest // 3, t // 3, :, t % 3 * 128 : t % 3 * 128 + 128]
        return tile if index % 2 == high else pltpu.roll(tile, 64, 1)

    for t in range(18):
        o_gqkv[:, 128 * t : 128 * t + 128] = jnp.where(
            low, packed_half(2 * t, 0), packed_half(2 * t + 1, 1)
        )
    got(S.early + 3, r.early_all.at[0])
    got(S.late + 3, r.late_all.at[0])
    early_rows = [early_steps[4](k) for k in range(4)]
    late_rows = [late_steps[4](k) for k in range(4)]
    mods = []
    for k in range(4):
        early, late = early_rows[k], late_rows[k]
        rows = jnp.concatenate([late[1:3], early[1:5], jnp.zeros((2, 768), F32)], axis=0)
        for n in range(6):
            for m in range(6):
                r.dmod_flat[k, 6 * n + m : 6 * n + m + 1, :] = rows[
                    n : n + 1, 128 * m : 128 * m + 128
                ]
        mods.append(rows)
    gain = jnp.concatenate(
        [
            sum(late_rows[k][0:1] for k in range(4)),
            sum(early_rows[k][0:1] for k in range(4)),
            (mods[0] + mods[1] + mods[2] + mods[3])[0:6],
        ],
        axis=0,
    )
    mask_row = sum(late_rows[k][3:4] for k in range(4))
    gains = jnp.concatenate([gain, mask_row, jnp.zeros((7, 768), F32)], axis=0)
    masters = jnp.concatenate([i_vec[...], jnp.zeros((7, 768), F32)], axis=0)
    own = lax.rem(WIDTH - 24 * me, WIDTH)
    o_gvec[...] = pltpu.roll(gains, own, 1)[:, 0:128]
    o_vec[...] = pltpu.roll(masters, own, 1)[:, 0:128]
    r.mod_pad[...] = jnp.zeros((8, 384), F32)
    window = lax.div(wide * me, 128)
    for k in range(4):
        rows = r.dmod_flat[k, pl.ds(window, 3), :]
        for m in range(3):
            r.mod_pad[k : k + 1, 128 * m : 128 * m + 128] = rows[m : m + 1, :]
    o_dmod[...] = pltpu.roll(r.mod_pad[...], lax.rem(384 - lax.rem(wide * me, 128), 384), 1)[:, 0:256]
    small = jnp.sum(gain * gain) + jnp.sum(mask_row * mask_row)
    conds = [r.conds_all[k][0:1].astype(BF).astype(F32) for k in range(4)]
    for k in range(4):
        for m in range(k, 4):
            term = jnp.sum(mods[k] * mods[m]) * jnp.sum(conds[k] * conds[m])
            small += term if m == k else 2.0 * term
    got(S.sq, r.sq.at[0:31])
    total = r.sq[0]
    for k in range(1, ALL):
        total += r.sq[k]
    o_norm[...] = jnp.broadcast_to(jnp.sqrt(jnp.sum(total) + small), (8, 128))

    for drained in drains:
        drained()


def run_layer(*args):
    shapes = (
        ((ROWS, WIDTH), BF),
        ((ROWS, WIDTH), F32),
        ((8, 128), F32),
        ((24, 3 * WIDTH), F32),
        ((24, WIDTH), F32),
        ((24, 4 * WIDTH), F32),
        ((96, WIDTH), F32),
        ((8, 256), F32),
        ((16, 128), F32),
        ((16, 128), F32),
        ((8, 128), F32),
    )
    whole = pl.BlockSpec(memory_space=pltpu.VMEM)
    return pl.pallas_call(
        layer_kernel,
        out_shape=[jax.ShapeDtypeStruct(shape, kind) for shape, kind in shapes],
        in_specs=[pl.BlockSpec(memory_space=pl.ANY)] * len(args),
        out_specs=[whole] * len(shapes),
        scratch_shapes=[pltpu.VMEM(shape, kind) for shape, kind in SCRATCH.values()]
        + [pltpu.SMEM((3, 1), jnp.int32)]
        + [pltpu.SemaphoreType.DMA((SEM_COUNT,)), pltpu.SemaphoreType.DMA((SEM_COUNT,))],
        compiler_params=pltpu.CompilerParams(
            collective_id=0, has_side_effects=True, vmem_limit_bytes=60 * 1024 * 1024
        ),
    )(*args)


HELD = (2, 8, 9, 7, 10, 3, 4, 5, 6)


def finish_kernel(*refs):
    sources, outs, refs = refs[:28], refs[28:49], refs[49:]
    near, results, load_sems, store_sems = refs[:28], refs[28:46], refs[46], refs[47]
    norm, g_vec, own_vec, dmod, conds = near[:5]
    weights, moments = (own_vec, *near[9:14]), near[14:26]

    order = list(range(5)) + [14, 15, 9, 16, 17]
    for k in range(2, 6):
        order += [3 + k, 8 + k, 14 + 2 * k, 15 + 2 * k]
    loads = {}
    for n in order:
        source = sources[HELD[n]] if n < 9 else sources[n + 2]
        loads[n] = pltpu.make_async_copy(source, near[n], load_sems.at[n])
        loads[n].start()
    for n in (26, 27):
        loads[n] = pltpu.make_async_copy(sources[n - 26], near[n], load_sems.at[n])
        loads[n].start()
    for n in order[:10]:
        loads[n].wait()
    outs[2][0, 0] = norm[0, 0]
    clip = jnp.minimum(1.0, CLIP / (norm[0:1, 0:1] + 1e-06))
    wide, narrow = near[9].shape[0], moments[0].shape[1]
    rounded = conds[...].astype(BF).astype(F32)
    turned_mod = dmod[...].T
    g_ada = turned_mod[0:wide, 0:1] * rounded[0:1, :]
    for k in range(1, 4):
        g_ada += turned_mod[0:wide, k : k + 1] * rounded[k : k + 1, :]
    stores = []
    for k in range(6):
        if k > 1:
            for n in order[2 + 4 * k : 6 + 4 * k]:
                loads[n].wait()
        grad = g_vec[0:9, 0:narrow] if k == 0 else g_ada if k == 1 else near[3 + k][...]
        updated = adam_step(
            weights[k][...] if k else own_vec[0:9, 0:narrow],
            grad * clip,
            moments[2 * k][...],
            moments[2 * k + 1][...],
            RATE if k else RATE_VECTORS,
            DECAY if k else 0.0,
        )
        for n in range(3):
            at = 3 * k + n
            results[at][...] = updated[n]
            stores.append(pltpu.make_async_copy(results[at], outs[3 + at], store_sems.at[at]))
            stores[-1].start()
    for n in (26, 27):
        loads[n].wait()
        stores.append(pltpu.make_async_copy(near[n], outs[n - 26].at[0], store_sems.at[n - 8]))
        stores[-1].start()
    for copy in stores:
        copy.wait()


def run_finish(partial_results, weights, moments):
    shapes = [((1, ROWS, WIDTH), BF), ((1, ROWS, WIDTH), F32), ((1, 1), F32)]
    for moment in moments[::2]:
        shapes += [(moment.shape, F32)] * 3
    far = pl.BlockSpec(memory_space=pl.ANY)
    specs = [far] * len(shapes)
    specs[2] = pl.BlockSpec(memory_space=pltpu.SMEM)
    near = [partial_results[k] for k in HELD] + [*weights, *moments, *partial_results[:2]]
    args = (*partial_results, *weights, *moments)
    return pl.pallas_call(
        finish_kernel,
        out_shape=[jax.ShapeDtypeStruct(shape, kind) for shape, kind in shapes],
        in_specs=[far] * len(args),
        out_specs=specs,
        scratch_shapes=[pltpu.VMEM(array.shape, array.dtype) for array in near]
        + [pltpu.VMEM(shape, kind) for shape, kind in shapes[3:]]
        + [pltpu.SemaphoreType.DMA((28,)), pltpu.SemaphoreType.DMA((20,))],
        compiler_params=pltpu.CompilerParams(vmem_limit_bytes=60 * 1024 * 1024),
    )(*args)


def slices(
    tokens_in,
    cotangent,
    timesteps,
    span_start,
    span_len,
    vectors,
    w_ada,
    w_qkv,
    w_attn,
    w_in,
    w_out,
    m_vec,
    v_vec,
    m_ada,
    v_ada,
    m_qkv,
    v_qkv,
    m_attn,
    v_attn,
    m_in,
    v_in,
    m_out,
    v_out,
):
    partial_results = run_layer(
        timesteps,
        span_start,
        span_len,
        tokens_in,
        cotangent,
        vectors,
        w_ada.T,
        w_qkv,
        w_attn,
        w_in,
        w_out,
    )
    moments = (
        m_vec,
        v_vec,
        m_ada.T,
        v_ada.T,
        m_qkv,
        v_qkv,
        m_attn,
        v_attn,
        m_in,
        v_in,
        m_out,
        v_out,
    )
    results = run_finish(partial_results, (w_ada.T, w_qkv, w_attn, w_in, w_out), moments)
    ada_results = [result.T for result in results[6:9]]
    return (*results[:2], results[2].reshape(()), *results[3:6], *ada_results, *results[9:])


def solution(mesh):
    in_specs = (
        P("dp", "seq", None),
        P("dp", "seq", None),
        P("dp"),
        P("dp"),
        P("dp"),
        P(),
        P(None, ("dp", "seq")),
        P(("dp", "seq"), None),
        P(("dp", "seq"), None),
        P(("dp", "seq"), None),
        P(("dp", "seq"), None),
        P(None, ("dp", "seq")),
        P(None, ("dp", "seq")),
        P(None, ("dp", "seq")),
        P(None, ("dp", "seq")),
        P(("dp", "seq"), None),
        P(("dp", "seq"), None),
        P(("dp", "seq"), None),
        P(("dp", "seq"), None),
        P(("dp", "seq"), None),
        P(("dp", "seq"), None),
        P(("dp", "seq"), None),
        P(("dp", "seq"), None),
    )
    out_specs = (
        P("dp", "seq", None),
        P("dp", "seq", None),
        P(),
        P(None, ("dp", "seq")),
        P(None, ("dp", "seq")),
        P(None, ("dp", "seq")),
        P(None, ("dp", "seq")),
        P(None, ("dp", "seq")),
        P(None, ("dp", "seq")),
        P(("dp", "seq"), None),
        P(("dp", "seq"), None),
        P(("dp", "seq"), None),
        P(("dp", "seq"), None),
        P(("dp", "seq"), None),
        P(("dp", "seq"), None),
        P(("dp", "seq"), None),
        P(("dp", "seq"), None),
        P(("dp", "seq"), None),
        P(("dp", "seq"), None),
        P(("dp", "seq"), None),
        P(("dp", "seq"), None),
    )
    sizes = dict(mesh.shape)
    local = slices if (sizes["dp"], sizes["seq"]) == (4, 8) else plain
    return jax.shard_map(local, mesh=mesh, in_specs=in_specs, out_specs=out_specs, check_vma=False)
```

```python
from functools import partial
import math
from types import SimpleNamespace

import jax
import jax.numpy as jnp
from jax import lax
from jax.experimental import pallas as pl
from jax.experimental.pallas import tpu as pltpu
from jax.sharding import PartitionSpec as P

HD = 64
COND = 128
STEP = 10


BETA_ONE = 0.9
BETA_TWO = 0.999
ADAM_EPS = 1e-08
RATE = 0.1
RATE_VECTORS = 0.3
DECAY = 0.01
CLIP = 1.0
NORM_EPS = 1e-05


def cond_input(timesteps):
    half_cond = COND // 2
    freqs = jnp.exp(jnp.arange(half_cond, dtype=jnp.float32) * (-math.log(10000.0) / half_cond))
    angles = timesteps.astype(jnp.float32)[:, None] * freqs[None, :]
    return jax.nn.silu(jnp.concatenate([jnp.cos(angles), jnp.sin(angles)], axis=1))


def rotary_tables(positions):
    half_head = HD // 2
    inverse = jnp.exp(jnp.arange(half_head, dtype=jnp.float32) * (-math.log(10000.0) / half_head))
    angles = positions.astype(jnp.float32)[:, None] * inverse[None, :]
    return (jnp.cos(angles), jnp.sin(angles))


def rotate(values, cosines, sines):
    half_head = values.shape[-1] // 2
    first = values[..., :half_head]
    second = values[..., half_head:]
    cos_b = cosines[:, None, :]
    sin_b = sines[:, None, :]
    return jnp.concatenate(
        [first * cos_b - second * sin_b, second * cos_b + first * sin_b], axis=-1
    )


def rotate_back(grads, cosines, sines):
    half_head = grads.shape[-1] // 2
    first = grads[..., :half_head]
    second = grads[..., half_head:]
    cos_b = cosines[:, None, :]
    sin_b = sines[:, None, :]
    return jnp.concatenate(
        [first * cos_b + second * sin_b, second * cos_b - first * sin_b], axis=-1
    )


def normalize(values):
    centre = jnp.mean(values, axis=-1, keepdims=True)
    centred = values - centre
    inverse = lax.rsqrt(jnp.mean(centred * centred, axis=-1, keepdims=True) + NORM_EPS)
    return (centred * inverse, inverse)


def norm_back(normed, inverse, grad):
    return inverse * (
        grad
        - jnp.mean(grad, axis=-1, keepdims=True)
        - normed * jnp.mean(grad * normed, axis=-1, keepdims=True)
    )


def split_kv(block, width):
    seqs, block_rows = (block.shape[0], block.shape[1])
    keys = block[..., :width].reshape(seqs, block_rows, width // HD, HD)
    values = block[..., width:].reshape(seqs, block_rows, width // HD, HD)
    return (keys, values)


def attend_piece(carry, piece, queries, width, factor):
    piece_rows = piece.shape[1]
    size = math.gcd(piece_rows, 512)

    def attend_one_block(index, state):
        running, denom, accum = state
        block = lax.dynamic_slice_in_dim(piece, index * size, size, 1)
        keys, values = split_kv(block, width)
        scores = (
            jnp.einsum("sqhd,skhd->shqk", queries, keys, preferred_element_type=jnp.float32)
            * factor
        )
        highest = jnp.maximum(running, jnp.max(scores, axis=-1))
        shrink = jnp.exp(running - highest)
        weights = jnp.exp(scores - highest[..., None])
        denom = denom * shrink + jnp.sum(weights, axis=-1)
        accum = accum * shrink[..., None] + jnp.einsum(
            "shqk,skhd->shqd",
            weights.astype(jnp.bfloat16),
            values,
            preferred_element_type=jnp.float32,
        )
        return (highest, denom, accum)

    return lax.fori_loop(0, piece_rows // size, attend_one_block, carry)


def block_grads(block, queries, grad_out, logsum, delta, width, factor):
    keys, values = split_kv(block, width)
    scores = (
        jnp.einsum("sqhd,skhd->shqk", queries, keys, preferred_element_type=jnp.float32) * factor
    )
    probs = jnp.exp(scores - logsum[..., None])
    dprobs = jnp.einsum("sqhd,skhd->shqk", grad_out, values, preferred_element_type=jnp.float32)
    dscores = (probs * (dprobs - delta[..., None])).astype(jnp.bfloat16)
    return (keys, probs, dscores)


def query_grads(kv_all, queries, grad_out, logsum, delta, width, factor):
    total_rows = kv_all.shape[1]
    size = math.gcd(total_rows, 512)

    def query_one_block(index, accum):
        block = lax.dynamic_slice_in_dim(kv_all, index * size, size, 1)
        keys, probs, dscores = block_grads(block, queries, grad_out, logsum, delta, width, factor)
        return accum + factor * jnp.einsum(
            "shqk,skhd->sqhd", dscores, keys, preferred_element_type=jnp.float32
        )

    return lax.fori_loop(
        0, total_rows // size, query_one_block, jnp.zeros(queries.shape, jnp.float32)
    )


def key_grads(kv_all, queries, grad_out, logsum, delta, width, factor, count):
    size = math.gcd(count, 512)
    seqs = queries.shape[0]

    def key_one_block(index, accum):
        block = lax.dynamic_slice_in_dim(kv_all, index * size, size, 1)
        keys, probs, dscores = block_grads(block, queries, grad_out, logsum, delta, width, factor)
        grad_vals = jnp.einsum(
            "shqk,sqhd->skhd",
            probs.astype(jnp.bfloat16),
            grad_out,
            preferred_element_type=jnp.float32,
        )
        grad_keys = factor * jnp.einsum(
            "shqk,sqhd->skhd", dscores, queries, preferred_element_type=jnp.float32
        )
        joined = jnp.concatenate(
            [grad_keys.reshape(seqs, size, width), grad_vals.reshape(seqs, size, width)], axis=-1
        )
        return lax.dynamic_update_slice_in_dim(
            accum, jnp.transpose(joined, (1, 0, 2)), index * size, 0
        )

    initial = jnp.zeros((count, seqs, 2 * width), jnp.float32)
    return lax.fori_loop(0, count // size, key_one_block, initial)


def adam_step(weight, grad, first, second, rate, decay_rate):
    new_first = BETA_ONE * first + (1.0 - BETA_ONE) * grad
    new_second = BETA_TWO * second + (1.0 - BETA_TWO) * grad * grad
    fixed_first = new_first / (1.0 - BETA_ONE**STEP)
    fixed_second = new_second / (1.0 - BETA_TWO**STEP)
    new_weight = weight - rate * (
        fixed_first / (jnp.sqrt(fixed_second) + ADAM_EPS) + decay_rate * weight
    )
    return (new_first, new_second, new_weight)


def mod_back(grad_hidden, ln_values, normed, scale_part, gain):
    grad_shift = jnp.sum(grad_hidden, axis=1)
    grad_scale = jnp.sum(grad_hidden * ln_values, axis=1)
    grad_ln = grad_hidden * (1.0 + scale_part)
    grad_gain = jnp.sum(grad_ln * normed, axis=(0, 1))
    return (grad_shift, grad_scale, grad_gain, grad_ln * gain)


def plain(
    tokens_in,
    cotangent,
    timesteps,
    span_start,
    span_len,
    vectors,
    w_ada,
    w_qkv,
    w_attn,
    w_in,
    w_out,
    m_vec,
    v_vec,
    m_ada,
    v_ada,
    m_qkv,
    v_qkv,
    m_attn,
    v_attn,
    m_in,
    v_in,
    m_out,
    v_out,
):
    seqs, group, width = tokens_in.shape
    heads = width // HD
    factor = HD ** (-0.5)
    flat_rows = seqs * group
    full_ada, full_qkv, full_attn, full_in, full_out = (
        lax.all_gather(w_ada.astype(jnp.bfloat16), ("dp", "seq"), axis=1, tiled=True),
        lax.all_gather(w_qkv.astype(jnp.bfloat16), ("dp", "seq"), axis=0, tiled=True),
        lax.all_gather(w_attn.astype(jnp.bfloat16), ("dp", "seq"), axis=0, tiled=True),
        lax.all_gather(w_in.astype(jnp.bfloat16), ("dp", "seq"), axis=0, tiled=True),
        lax.all_gather(w_out.astype(jnp.bfloat16), ("dp", "seq"), axis=0, tiled=True),
    )
    positions = lax.axis_index("seq") * group + jnp.arange(group, dtype=jnp.int32)
    masked = (positions[None, :] >= span_start[:, None]) & (
        positions[None, :] < (span_start + span_len)[:, None]
    )
    cond_bf = cond_input(timesteps).astype(jnp.bfloat16)
    modulation = jnp.dot(cond_bf, full_ada, preferred_element_type=jnp.float32) + vectors[
        2:8
    ].reshape(1, 6 * width)
    pieces = [modulation[:, which * width : (which + 1) * width][:, None, :] for which in range(6)]
    shift_one, scale_one, gate_one, shift_two, scale_two, gate_two = pieces
    start_tokens = jnp.where(
        masked[..., None], vectors[8][None, None, :], tokens_in.astype(jnp.float32)
    )
    normed_one, inv_one = normalize(start_tokens)
    ln_one = normed_one * vectors[0]
    hidden_one = (
        (ln_one * (1.0 + scale_one) + shift_one).astype(jnp.bfloat16).reshape(flat_rows, width)
    )
    projected = jnp.dot(hidden_one, full_qkv, preferred_element_type=jnp.float32).reshape(
        seqs, group, 3 * width
    )
    cosines, sines = rotary_tables(positions)
    queries = rotate(projected[..., :width].reshape(seqs, group, heads, HD), cosines, sines).astype(
        jnp.bfloat16
    )
    keys_here = rotate(
        projected[..., width : 2 * width].reshape(seqs, group, heads, HD), cosines, sines
    ).astype(jnp.bfloat16)
    values_here = projected[..., 2 * width :].astype(jnp.bfloat16)
    kv_local = jnp.concatenate([keys_here.reshape(seqs, group, width), values_here], axis=-1)
    initial = (
        jnp.full((seqs, heads, group), -1e30, jnp.float32),
        jnp.zeros((seqs, heads, group), jnp.float32),
        jnp.zeros((seqs, heads, group, HD), jnp.float32),
    )
    running, denom, accum = attend_piece(
        initial, lax.all_gather(kv_local, "seq", axis=1, tiled=True), queries, width, factor
    )
    attn_heads = accum / denom[..., None]
    logsum = running + jnp.log(denom)
    attn_rows = jnp.transpose(attn_heads, (0, 2, 1, 3)).reshape(flat_rows, width)
    attn_bf = attn_rows.astype(jnp.bfloat16)
    branch_one = jnp.dot(attn_bf, full_attn, preferred_element_type=jnp.float32).reshape(
        seqs, group, width
    )
    mid_tokens = start_tokens + gate_one * branch_one
    normed_two, inv_two = normalize(mid_tokens)
    ln_two = normed_two * vectors[1]
    hidden_two = (
        (ln_two * (1.0 + scale_two) + shift_two).astype(jnp.bfloat16).reshape(flat_rows, width)
    )
    pre_act = jnp.dot(hidden_two, full_in, preferred_element_type=jnp.float32)
    activ, gelu_back = jax.vjp(partial(jax.nn.gelu, approximate=True), pre_act)
    activ_bf = activ.astype(jnp.bfloat16)
    branch_two = jnp.dot(activ_bf, full_out, preferred_element_type=jnp.float32).reshape(
        seqs, group, width
    )
    block_out = (mid_tokens + gate_two * branch_two).astype(jnp.bfloat16)
    grad_y = cotangent.astype(jnp.float32)
    grad_gate_two = jnp.sum(grad_y * branch_two, axis=1)
    grad_branch_two = (grad_y * gate_two).astype(jnp.bfloat16).reshape(flat_rows, width)
    grad_w_out = jnp.dot(activ_bf.T, grad_branch_two, preferred_element_type=jnp.float32)
    grad_activ = jnp.dot(grad_branch_two, full_out.T, preferred_element_type=jnp.float32)
    grad_pre = gelu_back(grad_activ)[0].astype(jnp.bfloat16)
    grad_w_in = jnp.dot(hidden_two.T, grad_pre, preferred_element_type=jnp.float32)
    grad_hidden_two = jnp.dot(grad_pre, full_in.T, preferred_element_type=jnp.float32).reshape(
        seqs, group, width
    )
    grad_shift_two, grad_scale_two, grad_gain_two, grad_normed_two = mod_back(
        grad_hidden_two, ln_two, normed_two, scale_two, vectors[1]
    )
    grad_mid = grad_y + norm_back(normed_two, inv_two, grad_normed_two)
    grad_gate_one = jnp.sum(grad_mid * branch_one, axis=1)
    grad_branch_one = (grad_mid * gate_one).astype(jnp.bfloat16).reshape(flat_rows, width)
    grad_w_attn = jnp.dot(attn_bf.T, grad_branch_one, preferred_element_type=jnp.float32)
    grad_attn_bf = (
        jnp.dot(grad_branch_one, full_attn.T, preferred_element_type=jnp.float32)
        .astype(jnp.bfloat16)
        .reshape(seqs, group, heads, HD)
    )
    delta = jnp.einsum("sqhd,shqd->shq", grad_attn_bf.astype(jnp.float32), attn_heads)
    kv_all = lax.all_gather(kv_local, "seq", axis=1, tiled=True)
    grad_queries = query_grads(kv_all, queries, grad_attn_bf, logsum, delta, width, factor)
    grad_kv = jnp.transpose(
        lax.psum_scatter(
            key_grads(
                kv_all,
                queries,
                grad_attn_bf,
                logsum,
                delta,
                width,
                factor,
                group * lax.axis_size("seq"),
            ).astype(jnp.bfloat16),
            "seq",
            scatter_dimension=0,
            tiled=True,
        ).astype(jnp.float32),
        (1, 0, 2),
    )
    grad_keys = grad_kv[..., :width].reshape(seqs, group, heads, HD)
    grad_qkv = jnp.concatenate(
        [
            rotate_back(grad_queries, cosines, sines).reshape(seqs, group, width),
            rotate_back(grad_keys, cosines, sines).reshape(seqs, group, width),
            grad_kv[..., width:],
        ],
        axis=-1,
    )
    grad_qkv = grad_qkv.astype(jnp.bfloat16).reshape(flat_rows, 3 * width)
    grad_w_qkv = jnp.dot(hidden_one.T, grad_qkv, preferred_element_type=jnp.float32)
    grad_hidden_one = jnp.dot(grad_qkv, full_qkv.T, preferred_element_type=jnp.float32).reshape(
        seqs, group, width
    )
    grad_shift_one, grad_scale_one, grad_gain_one, grad_normed_one = mod_back(
        grad_hidden_one, ln_one, normed_one, scale_one, vectors[0]
    )
    grad_start = grad_mid + norm_back(normed_one, inv_one, grad_normed_one)
    grad_mask_row = jnp.sum(jnp.where(masked[..., None], grad_start, 0.0), axis=(0, 1))
    grad_input = jnp.where(masked[..., None], 0.0, grad_start)
    grad_mod = jnp.concatenate(
        [
            grad_shift_one,
            grad_scale_one,
            grad_gate_one,
            grad_shift_two,
            grad_scale_two,
            grad_gate_two,
        ],
        axis=1,
    )
    grad_w_ada = jnp.dot(cond_bf.astype(jnp.float32).T, grad_mod, precision=lax.Precision.HIGHEST)
    grad_vectors = jnp.concatenate(
        [
            grad_gain_one[None, :],
            grad_gain_two[None, :],
            jnp.sum(grad_mod, axis=0).reshape(6, width),
            grad_mask_row[None, :],
        ],
        axis=0,
    )
    red_ada, red_qkv, red_attn, red_in, red_out, red_vec = (
        lax.psum_scatter(grad_w_ada, ("dp", "seq"), scatter_dimension=1, tiled=True),
        lax.psum_scatter(grad_w_qkv, ("dp", "seq"), scatter_dimension=0, tiled=True),
        lax.psum_scatter(grad_w_attn, ("dp", "seq"), scatter_dimension=0, tiled=True),
        lax.psum_scatter(grad_w_in, ("dp", "seq"), scatter_dimension=0, tiled=True),
        lax.psum_scatter(grad_w_out, ("dp", "seq"), scatter_dimension=0, tiled=True),
        lax.psum_scatter(grad_vectors, ("dp", "seq"), scatter_dimension=1, tiled=True),
    )
    local_squares = jnp.float32(0.0)
    for reduced in (red_vec, red_ada, red_qkv, red_attn, red_in, red_out):
        local_squares = local_squares + jnp.sum(reduced * reduced)
    grad_norm = jnp.sqrt(lax.psum(local_squares, ("dp", "seq")))
    clip_factor = jnp.minimum(1.0, CLIP / (grad_norm + 1e-06))
    columns = red_vec.shape[1]
    own_vectors = lax.dynamic_slice_in_dim(
        vectors, lax.axis_index(("dp", "seq")) * columns, columns, 1
    )
    vec_out = adam_step(own_vectors, red_vec * clip_factor, m_vec, v_vec, RATE_VECTORS, 0.0)
    ada_out = adam_step(w_ada, red_ada * clip_factor, m_ada, v_ada, RATE, DECAY)
    qkv_out = adam_step(w_qkv, red_qkv * clip_factor, m_qkv, v_qkv, RATE, DECAY)
    attn_out = adam_step(w_attn, red_attn * clip_factor, m_attn, v_attn, RATE, DECAY)
    in_out = adam_step(w_in, red_in * clip_factor, m_in, v_in, RATE, DECAY)
    out_out = adam_step(w_out, red_out * clip_factor, m_out, v_out, RATE, DECAY)
    return (
        block_out,
        grad_input,
        grad_norm,
        vec_out[0],
        vec_out[1],
        vec_out[2],
        ada_out[0],
        ada_out[1],
        ada_out[2],
        qkv_out[0],
        qkv_out[1],
        qkv_out[2],
        attn_out[0],
        attn_out[1],
        attn_out[2],
        in_out[0],
        in_out[1],
        in_out[2],
        out_out[0],
        out_out[1],
        out_out[2],
    )


F32, BF = jnp.float32, jnp.bfloat16
MESH = pl.DeviceIdType.MESH
DP, LINE, SEQ, CHIPS, ALL = 4, 4, 8, 16, 32
ROWS, WIDTH, PACK = 128, 768, 640
HALF = WIDTH // 2
HALVES = ((0, 0), (0, 1), (0, 2), (2, 2), (1, 0), (1, 1), (1, 2), None, (2, 0), (2, 1))

def numbered(**counts):
    at = {}
    for name, count in counts.items():
        at[name] = sum(counts[other] for other in at)
    return SimpleNamespace(**at), sum(counts.values())


S, SEM_COUNT = numbered(
    load=11,
    cond=1,
    mix_qkv=1,
    mix_in=1,
    mix_attn=1,
    mod=1,
    w_qkv=1,
    w_attn=4,
    plane_in=1,
    w_in=4,
    w_out=4,
    group_qkv=4,
    group_attn=4,
    fw_qkv=1,
    fw_attn=1,
    fw_in=1,
    fw_out=1,
    tok=4,
    h2=4,
    dm=4,
    xf=4,
    o=1,
    mm=1,
    dh2=1,
    do=1,
    gp=1,
    dh1=5,
    pair_out=1,
    pair_in=1,
    pair_attn=1,
    pair_qkv=1,
    plane_attn=1,
    plane_qkv=1,
    line_out=5,
    line_in=5,
    slice_in=1,
    line_attn=1,
    line_qkv=1,
    last_in=1,
    last_attn=1,
    last_qkv=1,
    early=7,
    late=7,
    sq=1,
)

SCRATCH = dict(
    i_tok=((1, 128, 768), BF),
    i_cot=((1, 128, 768), BF),
    i_vec=((9, 768), F32),
    i_wada=((144, 128), F32),
    i_wqkv=((24, 2304), F32),
    i_wattn=((24, 768), F32),
    i_win=((24, 3072), F32),
    i_wout=((96, 768), F32),
    wide_qkv=((48, 3072), F32),
    wide_in=((48, 3072), F32),
    wide_attn=((48, 768), F32),
    s_qkv=((48, 3072), BF),
    s_in=((48, 3072), BF),
    s_attn=((48, 768), BF),
    w_qkv=((768, 768), BF),
    w_in=((4, 4, 48, 768), BF),
    w_attn=((768, 768), BF),
    w_out=((4, 2, 96, 768), BF),
    t_w_qkv=((640, 768), BF),
    t_w_attn=((768, 1024), BF),
    t_w_in=((768, 768), BF),
    t_w_out=((768, 768), BF),
    t_h1=((768, 512), BF),
    conds_all=((4, 8, 128), F32),
    mod_send=((4, 4, 128), F32),
    mod_got=((32, 4, 128), F32),
    mod_flat=((40, 128), F32),
    mod_pad=((8, 384), F32),
    turn=((2, 4, 128, 128), F32),
    dmod_flat=((4, 40, 128), F32),
    mod=((8, 768), F32),
    x0=((128, 768), F32),
    n1=((4, 128, 768), F32),
    inv1=((4, 128, 128), F32),
    x1=((128, 768), F32),
    n2=((128, 768), F32),
    inv2=((128, 128), F32),
    a=((128, 768), F32),
    dx1=((128, 768), F32),
    toks=((4, 128, 768), BF),
    h1=((4, 128, 768), BF),
    h2=((4, 128, 768), BF),
    dm=((4, 128, 768), BF),
    gb=((4, 128, 768), BF),
    du=((4, 128, 768), BF),
    xb=((2, 4, 128, 640), BF),
    pt=((3, 1024, 512), BF),
    vt=((2, 128, 1024), BF),
    kt=((2, 128, 1024), BF),
    back=((4, 128, 768), F32),
    ot=((2, 128, 512), F32),
    os=((4, 192, 128), BF),
    ob=((4, 192, 128), BF),
    o2=((4, 128, 128), BF),
    mms=((4, 128, 768), BF),
    mmr=((4, 128, 768), BF),
    dhs=((4, 128, 768), BF),
    dhr=((4, 128, 768), BF),
    das=((128, 768), BF),
    dos=((4, 192, 128), BF),
    dob=((4, 192, 128), BF),
    dst=((3, 1024, 512), BF),
    ga=((512, 640), F32),
    gps=((512, 512), BF),
    gpr=((512, 512), BF),
    dqkv=((4, 128, 768), BF),
    d1s=((4, 128, 768), BF),
    d1r=((4, 128, 768), BF),
    g_out=((4, 2, 96, 768), BF),
    g_in=((2, 4, 4, 48, 384), BF),
    g_attn=((2, 768, 384), BF),
    g_qkv=((2, 768, 384), BF),
    p_out=((4, 96, 768), BF),
    p_in=((4, 4, 48, 384), BF),
    p_attn=((768, 384), BF),
    p_qkv=((768, 384), BF),
    q_attn=((4, 192, 384), BF),
    q_qkv=((4, 192, 384), BF),
    m_attn=((192, 384), BF),
    m_qkv=((192, 384), BF),
    r_out=((4, 96, 768), BF),
    r_in=((4, 4, 48, 384), BF),
    via_in=((4, 48, 384), BF),
    via_out=((96, 768), BF),
    via_dh1=((128, 768), BF),
    m_in=((4, 48, 384), BF),
    u_in=((4, 48, 384), BF),
    r_attn=((4, 48, 384), BF),
    r_qkv=((4, 48, 384), BF),
    t_in=((4, 48, 384), F32),
    t_attn=((1, 48, 384), F32),
    t_qkv=((4, 48, 384), F32),
    f_in=((4, 2, 24, 384), F32),
    f_attn=((1, 2, 24, 384), F32),
    f_qkv=((4, 2, 24, 384), F32),
    early=((8, 768), F32),
    early_pair=((8, 768), F32),
    early_line=((4, 8, 384), F32),
    early_plane=((4, 8, 384), F32),
    early_all=((2, 4, 8, 384), F32),
    late=((4, 768), F32),
    late_pair=((4, 768), F32),
    late_line=((4, 4, 384), F32),
    late_plane=((4, 4, 384), F32),
    late_all=((2, 4, 4, 384), F32),
    sq=((32, 1, 128), F32),
)


def dot(left, right):
    return jnp.dot(left, right, preferred_element_type=F32)


def dot_nt(left, right):
    return lax.dot_general(left, right, (((1,), (1,)), ((), ())), preferred_element_type=F32)


def dot_tn(left, right):
    return lax.dot_general(left, right, (((0,), (0,)), ((), ())), preferred_element_type=F32)


def loop(count, body, start=0):
    def step(index, carry):
        body(index)
        return carry

    lax.fori_loop(start, count, step, 0)


def layer_kernel(
    i_time,
    i_start,
    i_len,
    h_tok,
    h_cot,
    h_vec,
    h_wada,
    h_wqkv,
    h_wattn,
    h_win,
    h_wout,
    o_y,
    o_dx,
    o_norm,
    o_gqkv,
    o_gattn,
    o_gin,
    o_gout,
    o_dmod,
    o_gvec,
    o_vec,
    o_conds,
    *scratch,
):
    r = SimpleNamespace(**dict(zip(SCRATCH, scratch)), when=scratch[-3])
    send_sems, recv_sems = scratch[-2:]
    i_tok, i_cot, i_vec, i_wada = r.i_tok, r.i_cot, r.i_vec, r.i_wada
    i_wqkv, i_wattn, i_win, i_wout = r.i_wqkv, r.i_wattn, r.i_win, r.i_wout
    b, s = lax.axis_index("dp"), lax.axis_index("seq")
    z, c = lax.div(s, 2), lax.rem(s, 2)
    mate = s + 1 - 2 * c
    chip = b * LINE + z
    me = b * SEQ + s
    drains = []

    def push(src, dst, at, to_b, to_s, out=None):
        pltpu.make_async_remote_copy(
            src_ref=src,
            dst_ref=dst,
            send_sem=send_sems.at[at if out is None else out],
            recv_sem=recv_sems.at[at],
            device_id=(to_b, to_s),
            device_id_type=MESH,
        ).start()

    def keep(src, dst, at):
        pltpu.make_async_copy(src, dst, recv_sems.at[at]).start()

    def got(at, like):
        pltpu.make_async_copy(like, like, recv_sems.at[at]).wait()

    def left(at, like):
        pltpu.make_async_copy(like, like, send_sems.at[at]).wait()

    def sent(at, like):
        drains.append(lambda: left(at, like))

    def by_core(body):
        for h, width in ((0, HALF), (1, PACK - HALF)):

            @pl.when(c == h)
            def _():
                body(slice(HALF * h, HALF * h + width), width)

    def sent_by_core(at, like):
        drains.append(lambda: by_core(lambda columns, width: left(at, like(width))))

    near = (b, b + 1 - 2 * lax.rem(b, 2), b + 2 - 4 * lax.div(b, 2), 3 - b)

    def toward(k):
        if k == 3:
            return 3, near[3]
        slot = 1 + c if k == 1 else 2 - c
        return slot, (1 - c) * near[k] + c * near[3 - k]

    def peers(body):
        for k in (1, 2, 3):
            body(*toward(k))

    def stack(body):
        for k in (1, 2, 3):
            body(lax.rem(z + k + 2 * c * (2 - k), LINE))

    def line_gather(block, at, near=True, rest=True):
        inner = 1 + lax.rem(z, 2)
        if near:
            push(block(z), block(z), at + z, b, 2 * inner + c, at)

        def one(to):
            relayed = ((z == 1) & (to == 3)) | ((z == 2) & (to == 0))

            @pl.when(jnp.logical_not(relayed | (to == inner)))
            def _():
                push(block(z), block(z), at + z, b, 2 * to + c, at)

        if rest:
            stack(one)

    def line_relay(block, at):
        for middle, source, to in ((2, 1, 3), (1, 2, 0)):

            @pl.when(z == middle)
            def _():
                got(at + source, block(source))
                push(block(source), block(source), at + source, b, 2 * to + c, at)

    def line_got(block, at, k):
        here = (k == z) | ((z == 2) & (k == 1)) | ((z == 1) & (k == 2))

        @pl.when(jnp.logical_not(here))
        def _():
            got(at + k, block(0))

    far = lax.div(z, 2)

    def line_order(j):
        return lax.rem(z + (2, 3 - 2 * far, 1 + 2 * far, 0)[j], LINE)

    def line_add(j, rows, dst, via, at):
        to = line_order(j)
        outer_chip = (z == 0) | (z == 3)

        def direct():
            push(rows(to), dst.at[z], at + z, b, 2 * to + c, at)

        if j == 0:

            @pl.when(outer_chip)
            def _():
                push(rows(to), via, at + 4, b, 2 * (1 + far) + c, at)

            @pl.when(jnp.logical_not(outer_chip))
            def _():
                direct()

        elif j < 3:
            direct()
        else:
            keep(rows(z), dst.at[z], at + z)

    def line_via(via, at, add):
        @pl.when((z == 1) | (z == 2))
        def _():
            got(at + 4, via)
            add()

    def line_done(dst, at):
        for k in range(4):
            missing = ((z == 1) & (k == 3)) | ((z == 2) & (k == 0))

            @pl.when(jnp.logical_not(missing))
            def _():
                got(at + k, dst.at[k])

    def line_clear(dst):
        for middle, k in ((1, 3), (2, 0)):

            @pl.when(z == middle)
            def _():
                dst[k] = jnp.zeros(dst.shape[1:], BF)

    lane = lax.broadcasted_iota(jnp.int32, (1, 128), 1)
    low = lane < 64
    own24 = pl.ds(pl.multiple_of(24 * c, 8), 24)
    mate24 = pl.ds(pl.multiple_of(24 * (1 - c), 8), 24)
    part = pl.ds(pl.multiple_of(HALF * c, 128), HALF)
    chip_rows = pl.ds(pl.multiple_of(48 * chip, 16), 48)
    group_rows = pl.ds(pl.multiple_of(192 * b, 16), 192)

    barrier = pltpu.get_barrier_semaphore()

    def greet(k):
        other = lax.rem(me + k, ALL)
        pl.semaphore_signal(
            barrier, inc=1, device_id=(lax.div(other, SEQ), lax.rem(other, SEQ)), device_id_type=MESH
        )

    loads = (
        (i_time, r.when.at[0]),
        (i_start, r.when.at[1]),
        (i_len, r.when.at[2]),
        (h_wqkv, i_wqkv),
        (h_win, i_win),
        (h_wattn, i_wattn),
        (h_wout, i_wout),
        (h_tok, i_tok),
        (h_vec, i_vec),
        (h_wada, i_wada),
        (h_cot, i_cot),
    )
    for k, (src, dst) in enumerate(loads):
        pltpu.make_async_copy(src, dst, recv_sems.at[S.load + k]).start()
    loop(ALL, greet, 1)
    for k, (src, dst) in enumerate(loads):
        pltpu.make_async_copy(src, dst, recv_sems.at[S.load + k]).wait()

    def natural(kind, p, head):
        return kind * WIDTH + 192 * p + 64 * head

    def half_at(ref, column, high):
        tile = ref[:, column // 128 * 128 : column // 128 * 128 + 128]
        return tile if (column % 128 == 64) == high else pltpu.roll(tile, 64, 1)

    for p in range(4):
        for tile in range(5):
            pair = []
            for high in (0, 1):
                which = HALVES[2 * tile + high]
                pair.append(
                    jnp.zeros((24, 128), F32)
                    if which is None
                    else half_at(i_wqkv, natural(which[0], p, which[1]), bool(high))
                )
            r.wide_qkv[own24, 768 * p + 128 * tile : 768 * p + 128 * tile + 128] = jnp.where(
                low, pair[0], pair[1]
            )
        r.wide_qkv[own24, 768 * p + 640 : 768 * p + 768] = jnp.zeros((24, 128), F32)
    r.wide_in[own24, :] = i_win[...]
    r.wide_attn[own24, :] = i_wattn[...]
    r.w_out[z, c] = i_wout[...].astype(BF)
    r.toks[z] = i_tok[0]
    line_clear(r.r_out)
    line_clear(r.r_in)
    line_clear(r.d1r)
    for ref in (r.q_qkv, r.r_qkv):
        ref[:, :, PACK - HALF : HALF] = jnp.zeros((4, ref.shape[1], WIDTH - PACK), BF)
    lanes8 = lax.broadcasted_iota(jnp.int32, (8, 128), 1)
    half_cond = COND // 2
    speed = jnp.exp((lanes8 % half_cond).astype(F32) * (-math.log(10000.0) / half_cond))
    angle = r.when[0, 0].astype(F32) * speed
    wave = jnp.where(lanes8 < half_cond, jnp.cos(angle), jnp.sin(angle))
    r.conds_all[b] = wave * (1.0 / (1.0 + jnp.exp(-wave)))
    pl.semaphore_wait(barrier, ALL - 1)

    def token_block(k):
        return r.toks.at[k]

    def attn_block(k):
        return r.w_attn.at[pl.ds(pl.multiple_of(192 * b + 48 * k, 16), 48), part]

    def in_block(k):
        return r.w_in.at[:, k, :, part]

    def out_block(k):
        return r.w_out.at[k, c]

    peers(lambda k, to: push(r.conds_all.at[b], r.conds_all.at[b], S.cond, to, s))
    sent(S.cond, r.conds_all.at[0:3])
    push(r.wide_qkv.at[own24], r.wide_qkv.at[own24], S.mix_qkv, b, mate)
    sent(S.mix_qkv, r.wide_qkv.at[0:24])
    push(r.wide_attn.at[own24], r.wide_attn.at[own24], S.mix_attn, b, mate)
    sent(S.mix_attn, r.wide_attn.at[0:24])
    push(r.wide_in.at[own24], r.wide_in.at[own24], S.mix_in, b, mate)
    sent(S.mix_in, r.wide_in.at[0:24])

    got(S.cond, r.conds_all.at[0:3])
    row8 = lax.broadcasted_iota(jnp.int32, (8, 128), 0)
    cond4 = jnp.zeros((8, 128), F32)
    for k in range(4):
        cond4 = jnp.where(row8 == k, r.conds_all[k], cond4)
    o_conds[...] = cond4
    wide = i_wada.shape[0]
    r.mod_pad[...] = jnp.zeros((8, 384), F32)
    r.mod_pad[:, 0:wide] = dot_nt(cond4.astype(BF), i_wada[...].astype(BF))
    columns = pltpu.roll(r.mod_pad[...], lax.rem(wide * me, 128), 1)
    for k in range(4):
        for t in range(3):
            r.mod_send[k, t : t + 1, :] = columns[k : k + 1, 128 * t : 128 * t + 128]
        r.mod_send[k, 3:4, :] = jnp.zeros((1, 128), F32)

    def send_mod(k):
        other = lax.rem(me + k, ALL)
        ob = lax.div(other, SEQ)
        push(r.mod_send.at[ob], r.mod_got.at[me], S.mod, ob, lax.rem(other, SEQ))

    loop(ALL, send_mod, 1)
    sent(S.mod, r.mod_got.at[0:31])
    keep(r.mod_send.at[b], r.mod_got.at[me], S.mod)

    def block(src, first):
        return src.at[:, pl.ds(pl.multiple_of(first, 128), HALF)]

    def slices_along_line():
        def send(columns, width):
            def rows(to):
                first = pl.multiple_of(WIDTH * to + columns.start, 128)
                return r.s_qkv.at[:, pl.ds(first, width)]

            dst = r.w_qkv.at[chip_rows, columns]
            stack(lambda to: push(rows(to), dst, S.w_qkv, b, 2 * to + c))
            keep(rows(z), dst, S.w_qkv)

        by_core(send)
        sent_by_core(S.w_qkv, lambda width: r.w_qkv.at[0:144, 0:width])

    def over_plane(dst, at):
        rows = dst.at[group_rows, part]
        peers(lambda k, to: push(rows, rows, at + k, to, s))
        for k in (1, 2, 3):
            sent(at + k, dst.at[0:192, 0:HALF])

    def share(dst, at, onward):
        for k in range(4):
            rows = dst.at[pl.ds(pl.multiple_of(192 * near[k], 16), 192), part]
            if k:
                got(at + k, rows)
            push(rows, rows, onward, b, mate)
        sent(onward, dst.at[:, 0:HALF])

    def line_share(block, at, onward):
        for k in range(4):
            line_got(block, at, k)
            push(block(k), block(k), onward, b, mate)

    got(S.mix_qkv, r.wide_qkv.at[0:24])
    r.s_qkv[...] = r.wide_qkv[...].astype(BF)
    slices_along_line()
    line_gather(token_block, S.tok, rest=False)
    sent(S.tok, r.toks.at[0:3])
    got(S.mix_attn, r.wide_attn.at[0:24])
    r.s_attn[...] = r.wide_attn[...].astype(BF)

    def qkv_over_plane(columns, width):
        got(S.w_qkv, r.w_qkv.at[0:192, 0:width])
        rows = r.w_qkv.at[group_rows, columns]
        peers(lambda k, to: push(rows, rows, S.group_qkv + k, to, s))

    by_core(qkv_over_plane)
    for k in (1, 2, 3):
        sent_by_core(S.group_qkv + k, lambda width: r.w_qkv.at[0:192, 0:width])
    line_gather(token_block, S.tok, near=False)
    for h in range(2):

        @pl.when(c == h)
        def _():
            r.w_attn[chip_rows, 384 * h : 384 * h + 384] = r.s_attn[:, 384 * h : 384 * h + 384]

    line_gather(attn_block, S.w_attn)
    sent(S.w_attn, r.w_attn.at[0:144, 0:HALF])
    line_gather(out_block, S.w_out)
    sent(S.w_out, r.w_out.at[0:3, 0])
    got(S.mix_in, r.wide_in.at[0:24])
    r.s_in[...] = r.wide_in[...].astype(BF)
    peers(
        lambda k, to: push(
            block(r.s_in, WIDTH * to + HALF * c), r.w_in.at[b, z, :, part], S.plane_in, to, s
        )
    )
    keep(block(r.s_in, WIDTH * b + HALF * c), r.w_in.at[b, z, :, part], S.plane_in)
    sent(S.plane_in, r.w_in.at[0:3, 0, :, 0:HALF])

    def hidden_rows(k):
        place = (2 * k + c) * ROWS + lax.broadcasted_iota(jnp.int32, (ROWS, 1), 0)
        return (place >= r.when[1, 0]) & (place < r.when[1, 0] + r.when[2, 0])

    def first_norm(tokens, k):
        x0 = jnp.where(hidden_rows(k), i_vec[8:9, :], tokens.astype(F32))
        normed, inverse = normalize(x0)
        r.n1[k] = normed
        r.inv1[k] = jnp.broadcast_to(inverse, (ROWS, 128))
        return x0

    r.x0[...] = first_norm(i_tok[0], z)

    got(S.mod, r.mod_got)
    r.mod_flat[...] = jnp.zeros((40, 128), F32)
    for k in range(ALL):
        first = 9 * k // 8
        r.mod_flat[first : first + 3, :] += r.mod_got[k, 0:3, :]
    for k in range(6):
        row = jnp.concatenate(
            [r.mod_flat[6 * k + t : 6 * k + t + 1, :] for t in range(6)], axis=1
        )
        r.mod[k : k + 1, :] = row + i_vec[2 + k : 3 + k, :]

    def mod(k):
        return r.mod[k : k + 1, :]

    def vec(k):
        return i_vec[k : k + 1, :]

    r.h1[z] = (r.n1[z] * vec(0) * (1.0 + mod(1)) + mod(0)).astype(BF)
    r.dm[0] = (i_cot[0].astype(F32) * mod(5)).astype(BF)
    peers(lambda k, to: push(r.dm.at[0], r.dm.at[k], S.dm + k, to, s))
    for k in (1, 2, 3):
        sent(S.dm + k, r.dm.at[0])

    lanes = lax.broadcasted_iota(jnp.int32, (ROWS, 128), 1)
    first_half = lanes % HD < HD // 2
    speed = jnp.exp((lanes % (HD // 2)).astype(F32) * (-math.log(10000.0) / (HD // 2)))
    row = lax.broadcasted_iota(jnp.int32, (ROWS, 128), 0)

    def table(k):
        angle = ((2 * k + c) * ROWS + row).astype(F32) * speed
        r.turn[0, k] = jnp.cos(angle)
        sine = jnp.sin(angle)
        r.turn[1, k] = jnp.where(first_half, -sine, sine)

    loop(LINE, table)

    line_relay(token_block, S.tok)

    def qkv_share(columns, width):
        for k in range(4):
            rows = r.w_qkv.at[pl.ds(pl.multiple_of(192 * near[k], 16), 192), columns]
            if k:
                got(S.group_qkv + k, rows)
            push(rows, rows, S.fw_qkv, b, mate)

    by_core(qkv_share)
    sent_by_core(S.fw_qkv, lambda width: r.w_qkv.at[:, 0:width])
    by_core(lambda columns, width: got(S.fw_qkv, r.w_qkv.at[:, 0 : PACK - width]))
    for k in range(5):
        columns = slice(128 * k, 128 * k + 128)
        r.t_w_qkv[columns, :] = r.w_qkv[:, columns].T

    def turned(tile, sign, k):
        other = jnp.where(first_half, pltpu.roll(tile, 96, 1), pltpu.roll(tile, 32, 1))
        return tile * r.turn[0, k] + sign * (other * r.turn[1, k])

    def project(j):
        k = lax.rem(z + j, LINE)

        @pl.when(j > 0)
        def _():
            line_got(token_block, S.tok, k)
            first_norm(r.toks[k], k)
            r.h1[k] = (r.n1[k] * vec(0) * (1.0 + mod(1)) + mod(0)).astype(BF)

        x = dot(r.h1[k], r.w_qkv[:, 0:PACK])
        tiles = [x[:, 128 * t : 128 * t + 128] for t in range(5)]
        tiles[0] = turned(tiles[0], 1.0, k) * 0.125
        tiles[1] = jnp.where(low, turned(tiles[1], 1.0, k) * 0.125, tiles[1])
        tiles[2] = turned(tiles[2], 1.0, k)
        tiles[3] = turned(tiles[3], 1.0, k)
        for t in range(5):
            r.xb[0, k, :, 128 * t : 128 * t + 128] = tiles[t].astype(BF)
        push(r.xb.at[0, k], r.xb.at[1, k], S.xf + k, b, mate)

    loop(4, project)
    line_relay(attn_block, S.w_attn)
    for k in range(4):
        line_got(attn_block, S.w_attn, k)
    over_plane(r.w_attn, S.group_attn)
    for k in range(4):
        sent(S.xf + k, r.xb.at[0, 0])

    for k in range(6):
        columns = slice(128 * k, 128 * k + 128)
        r.t_h1[columns, :] = r.h1[:, :, columns].reshape(512, 128).T
    for k in range(4):
        got(S.xf + k, r.xb.at[0, 0])

    def tile_of(t):
        return r.xb[:, :, :, 128 * t : 128 * t + 128].reshape(1024, 128)

    heads = ((0, 2, 4, True, True), (0, 2, 4, False, False), (1, 3, 1, True, False))

    def queries(head, first, size):
        q_tile, _, _, q_low, _ = heads[head]
        q = r.xb[0, first : first + size, :, 128 * q_tile : 128 * q_tile + 128]
        return jnp.where(low if q_low else ~low, q.reshape(size * 128, 128), jnp.zeros((), BF))

    r.vt[0] = tile_of(4).T
    r.vt[1] = tile_of(1).T
    for half in range(2):
        at = slice(256 * half, 256 * half + 256)
        for head in range(3):
            scores = dot_nt(tile_of(heads[head][1]), queries(head, 2 * half, 2))
            weights = jnp.exp(scores - jnp.max(scores, axis=0, keepdims=True))
            weights = weights * (1.0 / jnp.sum(weights, axis=0, keepdims=True))
            weights = weights.astype(BF)
            r.pt[head, :, at] = weights
            out = dot(r.vt[head // 2], weights)
            if head == 0:
                r.ot[0, 0:64, at] = out[0:64]
            elif head == 1:
                r.ot[0, 64:128, at] = out[64:128]
            else:
                r.ot[1, 0:64, at] = out[64:128]
                r.ot[1, 64:128, at] = jnp.zeros((64, 256), F32)
        for k in (2 * half, 2 * half + 1):
            across = slice(128 * k, 128 * k + 128)
            r.os[k, 0:128, :] = r.ot[0, :, across].T.astype(BF)
            third = r.ot[1, 0:64, across]
            third = jnp.concatenate([third, pltpu.roll(third, 64, 1)], axis=0)
            r.os[k, 128:192, :] = third.T[0:64].astype(BF)
        for to in (2 * half, 2 * half + 1):

            @pl.when(z == to)
            def _():
                keep(r.os.at[to], r.ob.at[z], S.o)

            @pl.when(z != to)
            def _():
                push(r.os.at[to], r.ob.at[z], S.o, b, 2 * to + c)

        if half == 0:
            line_relay(out_block, S.w_out)

    sent(S.o, r.os.at[0:3])
    got(S.plane_in, r.w_in.at[:, 0, :, 0:HALF])
    line_gather(in_block, S.w_in)
    sent(S.w_in, r.w_in.at[0:3, :, :, 0:HALF])
    for k in range(2):
        r.kt[k] = tile_of(2 + k).T
    share(r.w_attn, S.group_attn, S.fw_attn)
    got(S.fw_attn, r.w_attn.at[:, 0:HALF])
    for p in range(4):
        first = 192 * p
        r.t_w_attn[:, 256 * p : 256 * p + 128] = r.w_attn[first : first + 128, :].T
        third = r.w_attn[first + 128 : first + 192, :]
        r.t_w_attn[:, 256 * p + 128 : 256 * p + 256] = jnp.concatenate(
            [third, jnp.zeros_like(third)], axis=0
        ).T
    got(S.o, r.ob)
    a = jnp.zeros((ROWS, WIDTH), F32)
    for p in range(4):
        third = r.ob[p, 128:192, :].astype(F32)
        third = jnp.concatenate([third, pltpu.roll(third, 64, 1)], axis=0)
        r.o2[p] = jnp.where(low, third, 0.0).astype(BF)
        a += dot(r.ob[p, 0:128, :], r.w_attn[192 * p : 192 * p + 128, :])
        a += dot(r.o2[p, :, 0:64], r.w_attn[192 * p + 128 : 192 * p + 192, :])
    r.a[...] = a
    x1 = r.x0[...] + mod(2) * a
    r.x1[...] = x1
    n2, inv2 = normalize(x1)
    r.n2[...] = n2
    r.inv2[...] = jnp.broadcast_to(inv2, (ROWS, 128))
    r.h2[0] = (n2 * vec(1) * (1.0 + mod(4)) + mod(3)).astype(BF)
    peers(lambda k, to: push(r.h2.at[0], r.h2.at[k], S.h2 + k, to, s))
    for k in (1, 2, 3):
        sent(S.h2 + k, r.h2.at[0])
    line_relay(in_block, S.w_in)
    line_share(out_block, S.w_out, S.fw_out)
    sent(S.fw_out, r.w_out.at[:, 0])
    got(S.fw_out, r.w_out.at[:, 0])

    for k in range(6):
        columns = slice(128 * k, 128 * k + 128)
        r.t_w_out[columns, :] = r.w_out[:, :, :, columns].reshape(WIDTH, 128).T

    def feed_back(k):
        @pl.when(k > 0)
        def _():
            got(S.dm + k, r.dm.at[0])

        r.back[k] = dot(r.dm[k], r.t_w_out[...])

    loop(4, feed_back)
    line_share(in_block, S.w_in, S.fw_in)
    sent(S.fw_in, r.w_in.at[:, :, :, 0:HALF])
    got(S.fw_in, r.w_in.at[:, :, :, 0:HALF])
    for k in range(6):
        columns = slice(128 * k, 128 * k + 128)
        r.t_w_in[columns, :] = r.w_in[:, :, :, columns].reshape(WIDTH, 128).T

    def feed(first, count):
        at = slice(first, first + count)
        size = count * ROWS
        u = dot(r.h2[at].reshape(size, WIDTH), r.w_in[...].reshape(WIDTH, WIDTH))
        slope = 0.7978845608028654
        cube = 0.044715
        t = jnp.tanh(slope * (u + cube * u * u * u))
        r.gb[at] = (0.5 * u * (1.0 + t)).astype(BF).reshape(count, ROWS, WIDTH)
        bend = 0.5 * (1.0 + t) + 0.5 * u * (1.0 - t * t) * (slope * (1.0 + 3.0 * cube * u * u))
        du = (r.back[at].reshape(size, WIDTH) * bend).astype(BF)
        r.du[at] = du.reshape(count, ROWS, WIDTH)
        r.dhs[at] = dot(du, r.t_w_in[...]).astype(BF).reshape(count, ROWS, WIDTH)

    feed(0, 1)
    for first, count in ((1, 2), (3, 1)):
        for k in range(first, first + count):
            got(S.h2 + k, r.h2.at[0])
        feed(first, count)
        for k in range(first, first + count):
            slot, to = toward(k)
            push(r.dhs.at[slot], r.dhr.at[slot], S.dh2, to, s)
    sent(S.dh2, r.dhs.at[0:3])
    def gather(own, others):
        total = own[0].astype(F32)
        for k in (1, 2, 3):
            total += others[k].astype(F32)
        return total

    for k in range(2):
        rows = slice(384 * k, 384 * k + 384)
        result = dot_tn(r.gb[:, :, rows].reshape(512, 384), r.dm[...].reshape(512, 768))
        r.g_out[2 * k : 2 * k + 2] = result.astype(BF).reshape(2, 2, 96, 768)
    push(r.g_out.at[:, 1 - c], r.p_out, S.pair_out, b, mate)
    sent(S.pair_out, r.p_out)

    def to_mate(grad, dst, at):
        push(grad.at[1 - c], dst, at, b, mate)
        sent(at, dst)

    def pair_sum(grad, pair, at):
        got(at, pair)
        grad[c] = (grad[c].astype(F32) + pair[...].astype(F32)).astype(BF)

    def plane_sum(grad, dst, at, packed=False):
        def send(columns, width):
            def rows(to):
                return grad.at[c, pl.ds(pl.multiple_of(192 * to, 16), 192), 0:width]

            peers(lambda k, to: push(rows(to), dst.at[k, :, 0:width], at, to, s))
            keep(rows(b), dst.at[0, :, 0:width], at)

        if packed:
            by_core(send)
            sent_by_core(at, lambda width: dst.at[0:3, :, 0:width])
        else:
            send(None, HALF)
            sent(at, dst.at[0:3])

    def line_sum(src, total, dst, first, at, packed=False):
        def send(columns, width):
            got(first, src.at[:, :, 0:width])
            total[...] = (
                (src[0].astype(F32) + src[1].astype(F32))
                + (src[2].astype(F32) + src[3].astype(F32))
            ).astype(BF)

            def rows(to):
                return total.at[pl.ds(pl.multiple_of(48 * to, 16), 48), 0:width]

            stack(lambda to: push(rows(to), dst.at[z, :, 0:width], at, b, 2 * to + c))
            keep(rows(z), dst.at[z, :, 0:width], at)

        if packed:
            by_core(send)
            sent_by_core(at, lambda width: dst.at[0:3, :, 0:width])
        else:
            send(None, HALF)
            sent(at, dst.at[0:3])

    def trade(total, final, at):
        push(total.at[:, mate24], final.at[:, c], at, b, mate)
        sent(at, final.at[:, 0])
        final[:, c] = total[:, own24, :]

    def in_product(k):
        rows = slice(384 * k, 384 * k + 384)
        result = dot_tn(r.h2[:, :, rows].reshape(512, 384), r.du[...].reshape(512, 768)).astype(BF)
        for h in range(2):
            r.g_in[h, 2 * k : 2 * k + 2] = result[:, 384 * h : 384 * h + 384].reshape(2, 4, 48, 384)

    in_product(0)

    got(S.pair_out, r.p_out)
    for k in range(4):
        r.g_out[k, c] = (r.g_out[k, c].astype(F32) + r.p_out[k].astype(F32)).astype(BF)

    def out_rows(k):
        return r.g_out.at[k, c]

    for j in (0, 1):
        line_add(j, out_rows, r.r_out, r.via_out, S.line_out)
    in_product(1)
    to_mate(r.g_in, r.p_in, S.pair_in)

    def add_out():
        k = line_order(2)
        r.g_out[k, c] = (r.g_out[k, c].astype(F32) + r.via_out[...].astype(F32)).astype(BF)

    got(S.dh2, r.dhr.at[0:3])
    dh = gather(r.dhs, r.dhr)
    n2 = r.n2[...]
    inv2 = r.inv2[:, 0:1]
    r.early[...] = jnp.zeros((8, 768), F32)
    r.early[2:3, :] = jnp.sum(dh, axis=0, keepdims=True)
    both = jnp.sum(dh * n2, axis=0, keepdims=True)
    r.early[3:4, :] = both * vec(1)
    r.early[0:1, :] = both * (1.0 + mod(4))
    grad = dh * ((1.0 + mod(4)) * vec(1))
    dx1 = i_cot[0].astype(F32) + norm_back(n2, inv2, grad)
    r.dx1[...] = dx1
    r.early[1:2, :] = jnp.sum(dx1 * r.a[...], axis=0, keepdims=True)
    r.das[...] = (dx1 * mod(2)).astype(BF)
    def make_do(to):
        columns = pl.ds(pl.multiple_of(256 * to, 256), 256)
        result = dot(r.das[...], r.t_w_attn[:, columns])
        r.dos[to, 0:128, :] = result[:, 0:128].astype(BF)
        third = result[:, 128:256]
        third = jnp.where(low, third[0:64], pltpu.roll(third[64:128], 64, 1))
        r.dos[to, 128:192, :] = third.astype(BF)

    def send_do(to):
        make_do(to)
        push(r.dos.at[to], r.dob.at[z], S.do, b, 2 * to + c)

    stack(send_do)
    make_do(z)
    keep(r.dos.at[z], r.dob.at[z], S.do)
    sent(S.do, r.dos.at[0:3])
    for t in range(3):
        at = slice(256 * t, 256 * t + 256)
        mm = dot(r.gb[...].reshape(512, WIDTH), r.w_out[:, :, :, at].reshape(WIDTH, 256))
        r.mms[:, :, at] = mm.astype(BF).reshape(4, ROWS, 256)
    peers(lambda k, to: push(r.mms.at[k], r.mmr.at[k], S.mm, to, s))
    sent(S.mm, r.mms.at[0:3])

    for p in range(4):
        for rows, left_side in (
            (slice(192 * p, 192 * p + 128), r.ob[p, 0:128, :]),
            (slice(192 * p + 128, 192 * p + 192), r.o2[p]),
        ):
            result = dot_tn(left_side, r.das[...])[0 : rows.stop - rows.start].astype(BF)
            r.g_attn[0, rows, :] = result[:, 0:HALF]
            r.g_attn[1, rows, :] = result[:, HALF:WIDTH]
    to_mate(r.g_attn, r.p_attn, S.pair_attn)

    def small_sum(src, pair, line, plane, whole, at):
        def first():
            push(src, pair, at, b, mate)
            sent(at, src)

        def second():
            got(at, pair)
            total = src[...] + pair[...]
            line[z] = (1 - c) * total[:, 0:HALF] + c * total[:, HALF:WIDTH]
            stack(lambda to: push(line.at[z], line.at[z], at + 1, b, 2 * to + c))
            sent(at + 1, line.at[0:3])

        def third():
            got(at + 1, line.at[0:3])
            plane[b] = (line[0] + line[1]) + (line[2] + line[3])
            peers(lambda k, to: push(plane.at[b], plane.at[b], at + 2, to, s))
            sent(at + 2, plane.at[0:3])

        def fourth():
            got(at + 2, plane.at[0:3])
            whole[c] = plane[...]
            push(plane, whole.at[c], at + 3, b, mate)
            sent(at + 3, plane)

        def rows(k):
            return jnp.concatenate([whole[0, k], whole[1, k]], axis=1)

        return first, second, third, fourth, rows

    early_steps = small_sum(
        r.early, r.early_pair, r.early_line, r.early_plane, r.early_all, S.early
    )
    late_steps = small_sum(r.late, r.late_pair, r.late_line, r.late_plane, r.late_all, S.late)

    pair_sum(r.g_in, r.p_in, S.pair_in)
    line_via(r.via_out, S.line_out, add_out)
    for j in (2, 3):
        line_add(j, out_rows, r.r_out, r.via_out, S.line_out)
    sent(S.line_out, r.r_out.at[0:3])

    def in_rows(k):
        return r.g_in.at[c, :, k]

    for j in (0, 1):
        line_add(j, in_rows, r.r_in, r.via_in, S.line_in)

    def add_in():
        k = line_order(2)
        r.g_in[c, :, k] = (r.g_in[c, :, k].astype(F32) + r.via_in[...].astype(F32)).astype(BF)

    pair_sum(r.g_attn, r.p_attn, S.pair_attn)
    plane_sum(r.g_attn, r.q_attn, S.plane_attn)

    got(S.do, r.dob)
    dot0 = r.dob[:, 0:128, :].reshape(512, 128)
    third = r.dob[:, 128:192, :].astype(F32).reshape(256, 128)
    other_rows = jnp.where(low, pltpu.roll(third, 64, 1), 0.0).reshape(4, 64, 128)
    third = jnp.where(low, third, 0.0).reshape(4, 64, 128)
    dot1 = jnp.concatenate([third, other_rows], axis=1).reshape(512, 128)
    zero = jnp.zeros((), BF)
    moved = pltpu.roll(dot1, 64, 1).astype(BF)
    grads = (jnp.where(low, dot0, zero), jnp.where(low, zero, dot0), moved)
    product = dot0.astype(F32).T * r.ot[0]
    deltas = (
        jnp.sum(product[0:64], axis=0, keepdims=True),
        jnp.sum(product[64:128], axis=0, keepdims=True),
        jnp.sum(dot1.T * r.ot[1], axis=0, keepdims=True),
    )
    for head in range(3):
        values = tile_of(heads[head][2])
        for half in range(2):
            at = slice(256 * half, 256 * half + 256)
            dp = dot_nt(values, grads[head][at])
            r.dst[head, :, at] = (
                r.pt[head, :, at].astype(F32) * (dp - deltas[head][:, at])
            ).astype(BF)

    def key_grads(rows):
        dk = [dot(r.dst[head, rows, :], queries(head, 0, 4)) for head in range(3)]
        dv = [dot(r.pt[head, rows, :], grads[head]) for head in range(3)]
        return (dv[2], dk[0] + dk[1], dk[2], dv[0] + dv[1])

    for t, tile in enumerate(key_grads(slice(512, 1024))):
        r.gps[:, 128 * t : 128 * t + 128] = tile.astype(BF)
    push(r.gps, r.gpr, S.gp, b, mate)
    sent(S.gp, r.gps)
    for t, tile in enumerate(key_grads(slice(0, 512))):
        r.ga[:, 128 * t + 128 : 128 * t + 256] = tile
    for half in range(2):
        at = slice(256 * half, 256 * half + 256)
        turned_q = [dot(r.kt[head // 2], r.dst[head, :, at]) for head in range(3)]
        top = jnp.concatenate([turned_q[0][0:64], turned_q[1][64:128]], axis=0)
        r.ga[at, 0:128] = top.T * 0.125
        r.ga[at, 128:256] += turned_q[2].T * 0.125
    line_via(r.via_in, S.line_in, add_in)
    for j in (2, 3):
        line_add(j, in_rows, r.r_in, r.via_in, S.line_in)
    sent(S.line_in, r.r_in.at[0:3])
    got(S.gp, r.gpr)

    def dh1_rows(k):
        return r.d1s.at[k]

    def back_turn(k):
        rows = pl.ds(pl.multiple_of(128 * k, 128), 128)
        tiles = [r.ga[rows, 0:128]] + [
            r.ga[rows, 128 * t : 128 * t + 128]
            + r.gpr[rows, 128 * t - 128 : 128 * t].astype(F32)
            for t in range(1, 5)
        ]
        tiles[0] = turned(tiles[0], -1.0, k)
        tiles[1] = jnp.where(low, turned(tiles[1], -1.0, k), tiles[1])
        tiles[2] = turned(tiles[2], -1.0, k)
        tiles[3] = turned(tiles[3], -1.0, k)
        for t in range(5):
            r.dqkv[k, :, 128 * t : 128 * t + 128] = tiles[t].astype(BF)
        r.dqkv[k, :, PACK:WIDTH] = jnp.zeros((128, 128), BF)

    back_turn(line_order(0))

    def unproject(j):
        k = line_order(j)
        partial_sum = dot(r.dqkv[k, :, 0:PACK], r.t_w_qkv[...])
        r.d1s[k] = partial_sum.astype(BF)
        if j == 2:

            def add():
                r.d1s[k] = (partial_sum + r.via_dh1[...].astype(F32)).astype(BF)

            line_via(r.via_dh1, S.dh1, add)
        line_add(j, dh1_rows, r.d1r, r.via_dh1, S.dh1)
        n = r.n1[k]
        e = partial_sum * ((1.0 + mod(1)) * vec(0))
        weight = jnp.where(hidden_rows(k), r.inv1[k][:, 0:1], 0.0)
        centred = (
            e
            - jnp.mean(e, axis=-1, keepdims=True)
            - n * jnp.mean(e * n, axis=-1, keepdims=True)
        )
        r.late[0:1, :] += jnp.sum(partial_sum * n, axis=0, keepdims=True)
        r.late[1:2, :] += jnp.sum(partial_sum, axis=0, keepdims=True)
        r.late[3:4, :] += jnp.sum(weight * centred, axis=0, keepdims=True)

    r.late[...] = jnp.zeros((4, 768), F32)
    r.late[3:4, :] = jnp.sum(
        jnp.where(hidden_rows(z), r.dx1[...], 0.0), axis=0, keepdims=True
    )
    unproject(0)
    for j in (1, 2, 3):
        back_turn(line_order(j))

    def qkv_rows(k):
        rows = pl.ds(pl.multiple_of(128 * k, 128), 128)
        result = dot(r.t_h1[rows, :], r.dqkv[...].reshape(512, WIDTH)).astype(BF)
        r.g_qkv[0, rows, :] = result[:, 0:HALF]
        r.g_qkv[1, rows, :] = result[:, HALF:WIDTH]

    loop(6, qkv_rows)
    to_mate(r.g_qkv, r.p_qkv, S.pair_qkv)
    unproject(1)
    pair_sum(r.g_qkv, r.p_qkv, S.pair_qkv)
    plane_sum(r.g_qkv, r.q_qkv, S.plane_qkv, True)
    got(S.mm, r.mmr.at[0:3])
    mm = gather(r.mms, r.mmr)
    o_y[...] = (r.x1[...] + mod(5) * mm).astype(BF)
    r.early[4:5, :] = jnp.sum(i_cot[0].astype(F32) * mm, axis=0, keepdims=True)
    early_steps[0]()
    unproject(2)
    unproject(3)
    sent(S.dh1, r.d1s.at[0:3])
    both = r.late[0:1, :]
    r.late[2:3, :] = both * vec(0)
    r.late[0:1, :] = both * (1.0 + mod(1))
    late_steps[0]()
    early_steps[1]()
    line_sum(r.q_attn, r.m_attn, r.r_attn, S.plane_attn, S.line_attn)
    late_steps[1]()

    line_done(r.r_in, S.line_in)
    r.m_in[...] = (
        (r.r_in[0].astype(F32) + r.r_in[1].astype(F32))
        + (r.r_in[2].astype(F32) + r.r_in[3].astype(F32))
    ).astype(BF)
    peers(lambda k, to: push(r.m_in.at[to], r.u_in.at[b], S.slice_in, to, s))
    keep(r.m_in.at[b], r.u_in.at[b], S.slice_in)
    sent(S.slice_in, r.u_in.at[0:3])
    line_sum(r.q_qkv, r.m_qkv, r.r_qkv, S.plane_qkv, S.line_qkv, True)
    early_steps[2]()
    late_steps[2]()

    line_done(r.d1r, S.dh1)
    dh = (r.d1r[0].astype(F32) + r.d1r[1].astype(F32)) + (
        r.d1r[2].astype(F32) + r.d1r[3].astype(F32)
    )
    n1 = r.n1[z]
    grad = dh * ((1.0 + mod(1)) * vec(0))
    dx0 = r.dx1[...] + norm_back(n1, r.inv1[z][:, 0:1], grad)
    o_dx[...] = jnp.where(hidden_rows(z), 0.0, dx0)
    early_steps[3]()
    late_steps[3]()

    line_done(r.r_out, S.line_out)
    total = (r.r_out[0].astype(F32) + r.r_out[1].astype(F32)) + (
        r.r_out[2].astype(F32) + r.r_out[3].astype(F32)
    )
    o_gout[...] = total
    squares = total * total
    squares = jnp.sum(squares[:, 0:128] + squares[:, 128:256] + squares[:, 256:384]
                      + squares[:, 384:512] + squares[:, 512:640] + squares[:, 640:768],
                      axis=0, keepdims=True)

    def fold(value):
        total = value[:, 0:128] * value[:, 0:128]
        for t in range(1, value.shape[1] // 128):
            total += value[:, 128 * t : 128 * t + 128] * value[:, 128 * t : 128 * t + 128]
        return jnp.sum(total, axis=0, keepdims=True)

    got(S.slice_in, r.u_in)
    r.t_in[...] = r.u_in[...].astype(F32)
    for p in range(4):
        squares += fold(r.t_in[p])
    trade(r.t_in, r.f_in, S.last_in)
    got(S.line_attn, r.r_attn)
    r.t_attn[0] = (r.r_attn[0].astype(F32) + r.r_attn[1].astype(F32)) + (
        r.r_attn[2].astype(F32) + r.r_attn[3].astype(F32)
    )
    squares += fold(r.t_attn[0])
    trade(r.t_attn, r.f_attn, S.last_attn)
    by_core(lambda columns, width: got(S.line_qkv, r.r_qkv.at[:, :, 0:width]))
    r.t_qkv[...] = r.r_qkv[...].astype(F32)
    trade(r.t_qkv, r.f_qkv, S.last_qkv)
    for p in range(4):
        squares += fold(r.t_qkv[p])
    r.sq[me] = squares

    def send_sq(k):
        other = lax.rem(me + k, ALL)
        push(r.sq.at[me], r.sq.at[me], S.sq, lax.div(other, SEQ), lax.rem(other, SEQ))

    loop(ALL, send_sq, 1)
    sent(S.sq, r.sq.at[0:31])
    got(S.last_in, r.f_in.at[:, 0])
    got(S.last_attn, r.f_attn.at[:, 0])
    for h in range(2):
        for p in range(4):
            value = r.f_in[p, h]
            o_gin[:, 768 * p + 384 * h : 768 * p + 384 * h + 384] = value
        value = r.f_attn[0, h]
        o_gattn[:, 384 * h : 384 * h + 384] = value
    got(S.last_qkv, r.f_qkv.at[:, 0])
    where = {which: index for index, which in enumerate(HALVES) if which is not None}

    def packed_half(chunk, high):
        kind, rest = chunk // 12, chunk % 12
        index = where[(kind, rest % 3)]
        t = index // 2
        tile = r.f_qkv[rest // 3, t // 3, :, t % 3 * 128 : t % 3 * 128 + 128]
        return tile if index % 2 == high else pltpu.roll(tile, 64, 1)

    for t in range(18):
        o_gqkv[:, 128 * t : 128 * t + 128] = jnp.where(
            low, packed_half(2 * t, 0), packed_half(2 * t + 1, 1)
        )
    got(S.early + 3, r.early_all.at[0])
    got(S.late + 3, r.late_all.at[0])
    early_rows = [early_steps[4](k) for k in range(4)]
    late_rows = [late_steps[4](k) for k in range(4)]
    mods = []
    for k in range(4):
        early, late = early_rows[k], late_rows[k]
        rows = jnp.concatenate([late[1:3], early[1:5], jnp.zeros((2, 768), F32)], axis=0)
        for n in range(6):
            for m in range(6):
                r.dmod_flat[k, 6 * n + m : 6 * n + m + 1, :] = rows[
                    n : n + 1, 128 * m : 128 * m + 128
                ]
        mods.append(rows)
    gain = jnp.concatenate(
        [
            sum(late_rows[k][0:1] for k in range(4)),
            sum(early_rows[k][0:1] for k in range(4)),
            (mods[0] + mods[1] + mods[2] + mods[3])[0:6],
        ],
        axis=0,
    )
    mask_row = sum(late_rows[k][3:4] for k in range(4))
    gains = jnp.concatenate([gain, mask_row, jnp.zeros((7, 768), F32)], axis=0)
    masters = jnp.concatenate([i_vec[...], jnp.zeros((7, 768), F32)], axis=0)
    own = lax.rem(WIDTH - 24 * me, WIDTH)
    o_gvec[...] = pltpu.roll(gains, own, 1)[:, 0:128]
    o_vec[...] = pltpu.roll(masters, own, 1)[:, 0:128]
    r.mod_pad[...] = jnp.zeros((8, 384), F32)
    window = lax.div(wide * me, 128)
    for k in range(4):
        rows = r.dmod_flat[k, pl.ds(window, 3), :]
        for m in range(3):
            r.mod_pad[k : k + 1, 128 * m : 128 * m + 128] = rows[m : m + 1, :]
    o_dmod[...] = pltpu.roll(r.mod_pad[...], lax.rem(384 - lax.rem(wide * me, 128), 384), 1)[:, 0:256]
    small = jnp.sum(gain * gain) + jnp.sum(mask_row * mask_row)
    conds = [r.conds_all[k][0:1].astype(BF).astype(F32) for k in range(4)]
    for k in range(4):
        for m in range(k, 4):
            term = jnp.sum(mods[k] * mods[m]) * jnp.sum(conds[k] * conds[m])
            small += term if m == k else 2.0 * term
    got(S.sq, r.sq.at[0:31])
    total = r.sq[0]
    for k in range(1, ALL):
        total += r.sq[k]
    o_norm[...] = jnp.broadcast_to(jnp.sqrt(jnp.sum(total) + small), (8, 128))

    for drained in drains:
        drained()


def run_layer(*args):
    shapes = (
        ((ROWS, WIDTH), BF),
        ((ROWS, WIDTH), F32),
        ((8, 128), F32),
        ((24, 3 * WIDTH), F32),
        ((24, WIDTH), F32),
        ((24, 4 * WIDTH), F32),
        ((96, WIDTH), F32),
        ((8, 256), F32),
        ((16, 128), F32),
        ((16, 128), F32),
        ((8, 128), F32),
    )
    whole = pl.BlockSpec(memory_space=pltpu.VMEM)
    return pl.pallas_call(
        layer_kernel,
        out_shape=[jax.ShapeDtypeStruct(shape, kind) for shape, kind in shapes],
        in_specs=[pl.BlockSpec(memory_space=pl.ANY)] * len(args),
        out_specs=[whole] * len(shapes),
        scratch_shapes=[pltpu.VMEM(shape, kind) for shape, kind in SCRATCH.values()]
        + [pltpu.SMEM((3, 1), jnp.int32)]
        + [pltpu.SemaphoreType.DMA((SEM_COUNT,)), pltpu.SemaphoreType.DMA((SEM_COUNT,))],
        compiler_params=pltpu.CompilerParams(
            collective_id=0, has_side_effects=True, vmem_limit_bytes=60 * 1024 * 1024
        ),
    )(*args)


HELD = (2, 8, 9, 7, 10, 3, 4, 5, 6)


def finish_kernel(*refs):
    sources, outs, refs = refs[:28], refs[28:49], refs[49:]
    near, results, load_sems, store_sems = refs[:28], refs[28:46], refs[46], refs[47]
    norm, g_vec, own_vec, dmod, conds = near[:5]
    weights, moments = (own_vec, *near[9:14]), near[14:26]

    order = list(range(5)) + [14, 15, 9, 16, 17]
    for k in (4, 5, 2, 3):
        order += [3 + k, 8 + k, 14 + 2 * k, 15 + 2 * k]
    loads = {}
    for n in (26, 27):
        loads[n] = pltpu.make_async_copy(sources[n - 26], near[n], load_sems.at[n])
        loads[n].start()
    for n in order:
        source = sources[HELD[n]] if n < 9 else sources[n + 2]
        loads[n] = pltpu.make_async_copy(source, near[n], load_sems.at[n])
        loads[n].start()
    for n in order[:10]:
        loads[n].wait()
    outs[2][0, 0] = norm[0, 0]
    clip = jnp.minimum(1.0, CLIP / (norm[0:1, 0:1] + 1e-06))
    wide, narrow = near[9].shape[0], moments[0].shape[1]
    rounded = conds[...].astype(BF).astype(F32)
    turned_mod = dmod[...].T
    g_ada = turned_mod[0:wide, 0:1] * rounded[0:1, :]
    for k in range(1, 4):
        g_ada += turned_mod[0:wide, k : k + 1] * rounded[k : k + 1, :]
    stores = []
    for n in (26, 27):
        loads[n].wait()
        stores.append(pltpu.make_async_copy(near[n], outs[n - 26].at[0], store_sems.at[n - 8]))
        stores[-1].start()
    for step, k in enumerate((0, 1, 4, 5, 2, 3)):
        if step > 1:
            for n in order[2 + 4 * step : 6 + 4 * step]:
                loads[n].wait()
        grad = g_vec[0:9, 0:narrow] if k == 0 else g_ada if k == 1 else near[3 + k][...]
        updated = adam_step(
            weights[k][...] if k else own_vec[0:9, 0:narrow],
            grad * clip,
            moments[2 * k][...],
            moments[2 * k + 1][...],
            RATE if k else RATE_VECTORS,
            DECAY if k else 0.0,
        )
        for n in range(3):
            at = 3 * k + n
            results[at][...] = updated[n]
            stores.append(pltpu.make_async_copy(results[at], outs[3 + at], store_sems.at[at]))
            stores[-1].start()
    for copy in stores:
        copy.wait()


def run_finish(partial_results, weights, moments):
    shapes = [((1, ROWS, WIDTH), BF), ((1, ROWS, WIDTH), F32), ((1, 1), F32)]
    for moment in moments[::2]:
        shapes += [(moment.shape, F32)] * 3
    far = pl.BlockSpec(memory_space=pl.ANY)
    specs = [far] * len(shapes)
    specs[2] = pl.BlockSpec(memory_space=pltpu.SMEM)
    near = [partial_results[k] for k in HELD] + [*weights, *moments, *partial_results[:2]]
    args = (*partial_results, *weights, *moments)
    return pl.pallas_call(
        finish_kernel,
        out_shape=[jax.ShapeDtypeStruct(shape, kind) for shape, kind in shapes],
        in_specs=[far] * len(args),
        out_specs=specs,
        scratch_shapes=[pltpu.VMEM(array.shape, array.dtype) for array in near]
        + [pltpu.VMEM(shape, kind) for shape, kind in shapes[3:]]
        + [pltpu.SemaphoreType.DMA((28,)), pltpu.SemaphoreType.DMA((20,))],
        compiler_params=pltpu.CompilerParams(vmem_limit_bytes=60 * 1024 * 1024),
    )(*args)


def slices(
    tokens_in,
    cotangent,
    timesteps,
    span_start,
    span_len,
    vectors,
    w_ada,
    w_qkv,
    w_attn,
    w_in,
    w_out,
    m_vec,
    v_vec,
    m_ada,
    v_ada,
    m_qkv,
    v_qkv,
    m_attn,
    v_attn,
    m_in,
    v_in,
    m_out,
    v_out,
):
    partial_results = run_layer(
        timesteps,
        span_start,
        span_len,
        tokens_in,
        cotangent,
        vectors,
        w_ada.T,
        w_qkv,
        w_attn,
        w_in,
        w_out,
    )
    moments = (
        m_vec,
        v_vec,
        m_ada.T,
        v_ada.T,
        m_qkv,
        v_qkv,
        m_attn,
        v_attn,
        m_in,
        v_in,
        m_out,
        v_out,
    )
    results = run_finish(partial_results, (w_ada.T, w_qkv, w_attn, w_in, w_out), moments)
    ada_results = [result.T for result in results[6:9]]
    return (*results[:2], results[2].reshape(()), *results[3:6], *ada_results, *results[9:])


def solution(mesh):
    in_specs = (
        P("dp", "seq", None),
        P("dp", "seq", None),
        P("dp"),
        P("dp"),
        P("dp"),
        P(),
        P(None, ("dp", "seq")),
        P(("dp", "seq"), None),
        P(("dp", "seq"), None),
        P(("dp", "seq"), None),
        P(("dp", "seq"), None),
        P(None, ("dp", "seq")),
        P(None, ("dp", "seq")),
        P(None, ("dp", "seq")),
        P(None, ("dp", "seq")),
        P(("dp", "seq"), None),
        P(("dp", "seq"), None),
        P(("dp", "seq"), None),
        P(("dp", "seq"), None),
        P(("dp", "seq"), None),
        P(("dp", "seq"), None),
        P(("dp", "seq"), None),
        P(("dp", "seq"), None),
    )
    out_specs = (
        P("dp", "seq", None),
        P("dp", "seq", None),
        P(),
        P(None, ("dp", "seq")),
        P(None, ("dp", "seq")),
        P(None, ("dp", "seq")),
        P(None, ("dp", "seq")),
        P(None, ("dp", "seq")),
        P(None, ("dp", "seq")),
        P(("dp", "seq"), None),
        P(("dp", "seq"), None),
        P(("dp", "seq"), None),
        P(("dp", "seq"), None),
        P(("dp", "seq"), None),
        P(("dp", "seq"), None),
        P(("dp", "seq"), None),
        P(("dp", "seq"), None),
        P(("dp", "seq"), None),
        P(("dp", "seq"), None),
        P(("dp", "seq"), None),
        P(("dp", "seq"), None),
    )
    sizes = dict(mesh.shape)
    local = slices if (sizes["dp"], sizes["seq"]) == (4, 8) else plain
    return jax.shard_map(local, mesh=mesh, in_specs=in_specs, out_specs=out_specs, check_vma=False)
```

```python
from functools import partial
import math
from types import SimpleNamespace

import jax
import jax.numpy as jnp
from jax import lax
from jax.experimental import pallas as pl
from jax.experimental.pallas import tpu as pltpu
from jax.sharding import PartitionSpec as P

HD = 64
COND = 128
STEP = 10


BETA_ONE = 0.9
BETA_TWO = 0.999
ADAM_EPS = 1e-08
RATE = 0.1
RATE_VECTORS = 0.3
DECAY = 0.01
CLIP = 1.0
NORM_EPS = 1e-05


def cond_input(timesteps):
    half_cond = COND // 2
    freqs = jnp.exp(jnp.arange(half_cond, dtype=jnp.float32) * (-math.log(10000.0) / half_cond))
    angles = timesteps.astype(jnp.float32)[:, None] * freqs[None, :]
    return jax.nn.silu(jnp.concatenate([jnp.cos(angles), jnp.sin(angles)], axis=1))


def rotary_tables(positions):
    half_head = HD // 2
    inverse = jnp.exp(jnp.arange(half_head, dtype=jnp.float32) * (-math.log(10000.0) / half_head))
    angles = positions.astype(jnp.float32)[:, None] * inverse[None, :]
    return (jnp.cos(angles), jnp.sin(angles))


def rotate(values, cosines, sines):
    half_head = values.shape[-1] // 2
    first = values[..., :half_head]
    second = values[..., half_head:]
    cos_b = cosines[:, None, :]
    sin_b = sines[:, None, :]
    return jnp.concatenate(
        [first * cos_b - second * sin_b, second * cos_b + first * sin_b], axis=-1
    )


def rotate_back(grads, cosines, sines):
    half_head = grads.shape[-1] // 2
    first = grads[..., :half_head]
    second = grads[..., half_head:]
    cos_b = cosines[:, None, :]
    sin_b = sines[:, None, :]
    return jnp.concatenate(
        [first * cos_b + second * sin_b, second * cos_b - first * sin_b], axis=-1
    )


def normalize(values):
    centre = jnp.mean(values, axis=-1, keepdims=True)
    centred = values - centre
    inverse = lax.rsqrt(jnp.mean(centred * centred, axis=-1, keepdims=True) + NORM_EPS)
    return (centred * inverse, inverse)


def norm_back(normed, inverse, grad):
    return inverse * (
        grad
        - jnp.mean(grad, axis=-1, keepdims=True)
        - normed * jnp.mean(grad * normed, axis=-1, keepdims=True)
    )


def split_kv(block, width):
    seqs, block_rows = (block.shape[0], block.shape[1])
    keys = block[..., :width].reshape(seqs, block_rows, width // HD, HD)
    values = block[..., width:].reshape(seqs, block_rows, width // HD, HD)
    return (keys, values)


def attend_piece(carry, piece, queries, width, factor):
    piece_rows = piece.shape[1]
    size = math.gcd(piece_rows, 512)

    def attend_one_block(index, state):
        running, denom, accum = state
        block = lax.dynamic_slice_in_dim(piece, index * size, size, 1)
        keys, values = split_kv(block, width)
        scores = (
            jnp.einsum("sqhd,skhd->shqk", queries, keys, preferred_element_type=jnp.float32)
            * factor
        )
        highest = jnp.maximum(running, jnp.max(scores, axis=-1))
        shrink = jnp.exp(running - highest)
        weights = jnp.exp(scores - highest[..., None])
        denom = denom * shrink + jnp.sum(weights, axis=-1)
        accum = accum * shrink[..., None] + jnp.einsum(
            "shqk,skhd->shqd",
            weights.astype(jnp.bfloat16),
            values,
            preferred_element_type=jnp.float32,
        )
        return (highest, denom, accum)

    return lax.fori_loop(0, piece_rows // size, attend_one_block, carry)


def block_grads(block, queries, grad_out, logsum, delta, width, factor):
    keys, values = split_kv(block, width)
    scores = (
        jnp.einsum("sqhd,skhd->shqk", queries, keys, preferred_element_type=jnp.float32) * factor
    )
    probs = jnp.exp(scores - logsum[..., None])
    dprobs = jnp.einsum("sqhd,skhd->shqk", grad_out, values, preferred_element_type=jnp.float32)
    dscores = (probs * (dprobs - delta[..., None])).astype(jnp.bfloat16)
    return (keys, probs, dscores)


def query_grads(kv_all, queries, grad_out, logsum, delta, width, factor):
    total_rows = kv_all.shape[1]
    size = math.gcd(total_rows, 512)

    def query_one_block(index, accum):
        block = lax.dynamic_slice_in_dim(kv_all, index * size, size, 1)
        keys, probs, dscores = block_grads(block, queries, grad_out, logsum, delta, width, factor)
        return accum + factor * jnp.einsum(
            "shqk,skhd->sqhd", dscores, keys, preferred_element_type=jnp.float32
        )

    return lax.fori_loop(
        0, total_rows // size, query_one_block, jnp.zeros(queries.shape, jnp.float32)
    )


def key_grads(kv_all, queries, grad_out, logsum, delta, width, factor, count):
    size = math.gcd(count, 512)
    seqs = queries.shape[0]

    def key_one_block(index, accum):
        block = lax.dynamic_slice_in_dim(kv_all, index * size, size, 1)
        keys, probs, dscores = block_grads(block, queries, grad_out, logsum, delta, width, factor)
        grad_vals = jnp.einsum(
            "shqk,sqhd->skhd",
            probs.astype(jnp.bfloat16),
            grad_out,
            preferred_element_type=jnp.float32,
        )
        grad_keys = factor * jnp.einsum(
            "shqk,sqhd->skhd", dscores, queries, preferred_element_type=jnp.float32
        )
        joined = jnp.concatenate(
            [grad_keys.reshape(seqs, size, width), grad_vals.reshape(seqs, size, width)], axis=-1
        )
        return lax.dynamic_update_slice_in_dim(
            accum, jnp.transpose(joined, (1, 0, 2)), index * size, 0
        )

    initial = jnp.zeros((count, seqs, 2 * width), jnp.float32)
    return lax.fori_loop(0, count // size, key_one_block, initial)


def adam_step(weight, grad, first, second, rate, decay_rate):
    new_first = BETA_ONE * first + (1.0 - BETA_ONE) * grad
    new_second = BETA_TWO * second + (1.0 - BETA_TWO) * grad * grad
    fixed_first = new_first / (1.0 - BETA_ONE**STEP)
    fixed_second = new_second / (1.0 - BETA_TWO**STEP)
    new_weight = weight - rate * (
        fixed_first / (jnp.sqrt(fixed_second) + ADAM_EPS) + decay_rate * weight
    )
    return (new_first, new_second, new_weight)


def mod_back(grad_hidden, ln_values, normed, scale_part, gain):
    grad_shift = jnp.sum(grad_hidden, axis=1)
    grad_scale = jnp.sum(grad_hidden * ln_values, axis=1)
    grad_ln = grad_hidden * (1.0 + scale_part)
    grad_gain = jnp.sum(grad_ln * normed, axis=(0, 1))
    return (grad_shift, grad_scale, grad_gain, grad_ln * gain)


def plain(
    tokens_in,
    cotangent,
    timesteps,
    span_start,
    span_len,
    vectors,
    w_ada,
    w_qkv,
    w_attn,
    w_in,
    w_out,
    m_vec,
    v_vec,
    m_ada,
    v_ada,
    m_qkv,
    v_qkv,
    m_attn,
    v_attn,
    m_in,
    v_in,
    m_out,
    v_out,
):
    seqs, group, width = tokens_in.shape
    heads = width // HD
    factor = HD ** (-0.5)
    flat_rows = seqs * group
    full_ada, full_qkv, full_attn, full_in, full_out = (
        lax.all_gather(w_ada.astype(jnp.bfloat16), ("dp", "seq"), axis=1, tiled=True),
        lax.all_gather(w_qkv.astype(jnp.bfloat16), ("dp", "seq"), axis=0, tiled=True),
        lax.all_gather(w_attn.astype(jnp.bfloat16), ("dp", "seq"), axis=0, tiled=True),
        lax.all_gather(w_in.astype(jnp.bfloat16), ("dp", "seq"), axis=0, tiled=True),
        lax.all_gather(w_out.astype(jnp.bfloat16), ("dp", "seq"), axis=0, tiled=True),
    )
    positions = lax.axis_index("seq") * group + jnp.arange(group, dtype=jnp.int32)
    masked = (positions[None, :] >= span_start[:, None]) & (
        positions[None, :] < (span_start + span_len)[:, None]
    )
    cond_bf = cond_input(timesteps).astype(jnp.bfloat16)
    modulation = jnp.dot(cond_bf, full_ada, preferred_element_type=jnp.float32) + vectors[
        2:8
    ].reshape(1, 6 * width)
    pieces = [modulation[:, which * width : (which + 1) * width][:, None, :] for which in range(6)]
    shift_one, scale_one, gate_one, shift_two, scale_two, gate_two = pieces
    start_tokens = jnp.where(
        masked[..., None], vectors[8][None, None, :], tokens_in.astype(jnp.float32)
    )
    normed_one, inv_one = normalize(start_tokens)
    ln_one = normed_one * vectors[0]
    hidden_one = (
        (ln_one * (1.0 + scale_one) + shift_one).astype(jnp.bfloat16).reshape(flat_rows, width)
    )
    projected = jnp.dot(hidden_one, full_qkv, preferred_element_type=jnp.float32).reshape(
        seqs, group, 3 * width
    )
    cosines, sines = rotary_tables(positions)
    queries = rotate(projected[..., :width].reshape(seqs, group, heads, HD), cosines, sines).astype(
        jnp.bfloat16
    )
    keys_here = rotate(
        projected[..., width : 2 * width].reshape(seqs, group, heads, HD), cosines, sines
    ).astype(jnp.bfloat16)
    values_here = projected[..., 2 * width :].astype(jnp.bfloat16)
    kv_local = jnp.concatenate([keys_here.reshape(seqs, group, width), values_here], axis=-1)
    initial = (
        jnp.full((seqs, heads, group), -1e30, jnp.float32),
        jnp.zeros((seqs, heads, group), jnp.float32),
        jnp.zeros((seqs, heads, group, HD), jnp.float32),
    )
    running, denom, accum = attend_piece(
        initial, lax.all_gather(kv_local, "seq", axis=1, tiled=True), queries, width, factor
    )
    attn_heads = accum / denom[..., None]
    logsum = running + jnp.log(denom)
    attn_rows = jnp.transpose(attn_heads, (0, 2, 1, 3)).reshape(flat_rows, width)
    attn_bf = attn_rows.astype(jnp.bfloat16)
    branch_one = jnp.dot(attn_bf, full_attn, preferred_element_type=jnp.float32).reshape(
        seqs, group, width
    )
    mid_tokens = start_tokens + gate_one * branch_one
    normed_two, inv_two = normalize(mid_tokens)
    ln_two = normed_two * vectors[1]
    hidden_two = (
        (ln_two * (1.0 + scale_two) + shift_two).astype(jnp.bfloat16).reshape(flat_rows, width)
    )
    pre_act = jnp.dot(hidden_two, full_in, preferred_element_type=jnp.float32)
    activ, gelu_back = jax.vjp(partial(jax.nn.gelu, approximate=True), pre_act)
    activ_bf = activ.astype(jnp.bfloat16)
    branch_two = jnp.dot(activ_bf, full_out, preferred_element_type=jnp.float32).reshape(
        seqs, group, width
    )
    block_out = (mid_tokens + gate_two * branch_two).astype(jnp.bfloat16)
    grad_y = cotangent.astype(jnp.float32)
    grad_gate_two = jnp.sum(grad_y * branch_two, axis=1)
    grad_branch_two = (grad_y * gate_two).astype(jnp.bfloat16).reshape(flat_rows, width)
    grad_w_out = jnp.dot(activ_bf.T, grad_branch_two, preferred_element_type=jnp.float32)
    grad_activ = jnp.dot(grad_branch_two, full_out.T, preferred_element_type=jnp.float32)
    grad_pre = gelu_back(grad_activ)[0].astype(jnp.bfloat16)
    grad_w_in = jnp.dot(hidden_two.T, grad_pre, preferred_element_type=jnp.float32)
    grad_hidden_two = jnp.dot(grad_pre, full_in.T, preferred_element_type=jnp.float32).reshape(
        seqs, group, width
    )
    grad_shift_two, grad_scale_two, grad_gain_two, grad_normed_two = mod_back(
        grad_hidden_two, ln_two, normed_two, scale_two, vectors[1]
    )
    grad_mid = grad_y + norm_back(normed_two, inv_two, grad_normed_two)
    grad_gate_one = jnp.sum(grad_mid * branch_one, axis=1)
    grad_branch_one = (grad_mid * gate_one).astype(jnp.bfloat16).reshape(flat_rows, width)
    grad_w_attn = jnp.dot(attn_bf.T, grad_branch_one, preferred_element_type=jnp.float32)
    grad_attn_bf = (
        jnp.dot(grad_branch_one, full_attn.T, preferred_element_type=jnp.float32)
        .astype(jnp.bfloat16)
        .reshape(seqs, group, heads, HD)
    )
    delta = jnp.einsum("sqhd,shqd->shq", grad_attn_bf.astype(jnp.float32), attn_heads)
    kv_all = lax.all_gather(kv_local, "seq", axis=1, tiled=True)
    grad_queries = query_grads(kv_all, queries, grad_attn_bf, logsum, delta, width, factor)
    grad_kv = jnp.transpose(
        lax.psum_scatter(
            key_grads(
                kv_all,
                queries,
                grad_attn_bf,
                logsum,
                delta,
                width,
                factor,
                group * lax.axis_size("seq"),
            ).astype(jnp.bfloat16),
            "seq",
            scatter_dimension=0,
            tiled=True,
        ).astype(jnp.float32),
        (1, 0, 2),
    )
    grad_keys = grad_kv[..., :width].reshape(seqs, group, heads, HD)
    grad_qkv = jnp.concatenate(
        [
            rotate_back(grad_queries, cosines, sines).reshape(seqs, group, width),
            rotate_back(grad_keys, cosines, sines).reshape(seqs, group, width),
            grad_kv[..., width:],
        ],
        axis=-1,
    )
    grad_qkv = grad_qkv.astype(jnp.bfloat16).reshape(flat_rows, 3 * width)
    grad_w_qkv = jnp.dot(hidden_one.T, grad_qkv, preferred_element_type=jnp.float32)
    grad_hidden_one = jnp.dot(grad_qkv, full_qkv.T, preferred_element_type=jnp.float32).reshape(
        seqs, group, width
    )
    grad_shift_one, grad_scale_one, grad_gain_one, grad_normed_one = mod_back(
        grad_hidden_one, ln_one, normed_one, scale_one, vectors[0]
    )
    grad_start = grad_mid + norm_back(normed_one, inv_one, grad_normed_one)
    grad_mask_row = jnp.sum(jnp.where(masked[..., None], grad_start, 0.0), axis=(0, 1))
    grad_input = jnp.where(masked[..., None], 0.0, grad_start)
    grad_mod = jnp.concatenate(
        [
            grad_shift_one,
            grad_scale_one,
            grad_gate_one,
            grad_shift_two,
            grad_scale_two,
            grad_gate_two,
        ],
        axis=1,
    )
    grad_w_ada = jnp.dot(cond_bf.astype(jnp.float32).T, grad_mod, precision=lax.Precision.HIGHEST)
    grad_vectors = jnp.concatenate(
        [
            grad_gain_one[None, :],
            grad_gain_two[None, :],
            jnp.sum(grad_mod, axis=0).reshape(6, width),
            grad_mask_row[None, :],
        ],
        axis=0,
    )
    red_ada, red_qkv, red_attn, red_in, red_out, red_vec = (
        lax.psum_scatter(grad_w_ada, ("dp", "seq"), scatter_dimension=1, tiled=True),
        lax.psum_scatter(grad_w_qkv, ("dp", "seq"), scatter_dimension=0, tiled=True),
        lax.psum_scatter(grad_w_attn, ("dp", "seq"), scatter_dimension=0, tiled=True),
        lax.psum_scatter(grad_w_in, ("dp", "seq"), scatter_dimension=0, tiled=True),
        lax.psum_scatter(grad_w_out, ("dp", "seq"), scatter_dimension=0, tiled=True),
        lax.psum_scatter(grad_vectors, ("dp", "seq"), scatter_dimension=1, tiled=True),
    )
    local_squares = jnp.float32(0.0)
    for reduced in (red_vec, red_ada, red_qkv, red_attn, red_in, red_out):
        local_squares = local_squares + jnp.sum(reduced * reduced)
    grad_norm = jnp.sqrt(lax.psum(local_squares, ("dp", "seq")))
    clip_factor = jnp.minimum(1.0, CLIP / (grad_norm + 1e-06))
    columns = red_vec.shape[1]
    own_vectors = lax.dynamic_slice_in_dim(
        vectors, lax.axis_index(("dp", "seq")) * columns, columns, 1
    )
    vec_out = adam_step(own_vectors, red_vec * clip_factor, m_vec, v_vec, RATE_VECTORS, 0.0)
    ada_out = adam_step(w_ada, red_ada * clip_factor, m_ada, v_ada, RATE, DECAY)
    qkv_out = adam_step(w_qkv, red_qkv * clip_factor, m_qkv, v_qkv, RATE, DECAY)
    attn_out = adam_step(w_attn, red_attn * clip_factor, m_attn, v_attn, RATE, DECAY)
    in_out = adam_step(w_in, red_in * clip_factor, m_in, v_in, RATE, DECAY)
    out_out = adam_step(w_out, red_out * clip_factor, m_out, v_out, RATE, DECAY)
    return (
        block_out,
        grad_input,
        grad_norm,
        vec_out[0],
        vec_out[1],
        vec_out[2],
        ada_out[0],
        ada_out[1],
        ada_out[2],
        qkv_out[0],
        qkv_out[1],
        qkv_out[2],
        attn_out[0],
        attn_out[1],
        attn_out[2],
        in_out[0],
        in_out[1],
        in_out[2],
        out_out[0],
        out_out[1],
        out_out[2],
    )


F32, BF = jnp.float32, jnp.bfloat16
MESH = pl.DeviceIdType.MESH
DP, LINE, SEQ, CHIPS, ALL = 4, 4, 8, 16, 32
ROWS, WIDTH, PACK = 128, 768, 640
HALF = WIDTH // 2
HALVES = ((0, 0), (0, 1), (0, 2), (2, 2), (1, 0), (1, 1), (1, 2), None, (2, 0), (2, 1))

def numbered(**counts):
    at = {}
    for name, count in counts.items():
        at[name] = sum(counts[other] for other in at)
    return SimpleNamespace(**at), sum(counts.values())


S, SEM_COUNT = numbered(
    load=11,
    cond=1,
    mix_qkv=1,
    mix_in=1,
    mix_attn=1,
    mod=1,
    mod_pair=1,
    w_qkv=1,
    w_attn=4,
    plane_in=1,
    w_in=4,
    w_out=4,
    group_qkv=4,
    group_attn=4,
    fw_qkv=1,
    fw_attn=1,
    fw_in=1,
    fw_out=1,
    tok=4,
    h2=4,
    dm=4,
    xf=4,
    o=1,
    mm=1,
    dh2=1,
    do=1,
    gp=1,
    dh1=5,
    pair_out=1,
    pair_in=1,
    pair_attn=1,
    pair_qkv=1,
    plane_attn=1,
    plane_qkv=1,
    line_out=5,
    line_in=5,
    slice_in=1,
    line_attn=1,
    line_qkv=1,
    last_in=1,
    last_attn=1,
    last_qkv=1,
    early=7,
    late=7,
    sq=1,
)

SCRATCH = dict(
    i_tok=((1, 128, 768), BF),
    i_cot=((1, 128, 768), BF),
    i_vec=((9, 768), F32),
    i_wada=((144, 128), F32),
    i_wqkv=((24, 2304), F32),
    i_wattn=((24, 768), F32),
    i_win=((24, 3072), F32),
    i_wout=((96, 768), F32),
    wide_qkv=((48, 3072), F32),
    wide_in=((48, 3072), F32),
    wide_attn=((48, 768), F32),
    s_qkv=((48, 3072), BF),
    s_in=((48, 3072), BF),
    s_attn=((48, 768), BF),
    w_qkv=((768, 768), BF),
    w_in=((4, 4, 48, 768), BF),
    w_attn=((768, 768), BF),
    w_out=((4, 2, 96, 768), BF),
    t_w_qkv=((640, 768), BF),
    t_w_attn=((768, 1024), BF),
    t_w_in=((768, 768), BF),
    t_w_out=((768, 768), BF),
    t_h1=((768, 512), BF),
    conds_all=((4, 8, 128), F32),
    mod_send=((4, 4, 128), F32),
    mod_got=((2, 16, 4, 128), F32),
    mod_flat=((40, 128), F32),
    mod_pad=((8, 384), F32),
    turn=((2, 4, 128, 128), F32),
    dmod_flat=((4, 40, 128), F32),
    mod=((8, 768), F32),
    x0=((128, 768), F32),
    n1=((4, 128, 768), F32),
    inv1=((4, 128, 128), F32),
    x1=((128, 768), F32),
    n2=((128, 768), F32),
    inv2=((128, 128), F32),
    a=((128, 768), F32),
    dx1=((128, 768), F32),
    toks=((4, 128, 768), BF),
    h1=((4, 128, 768), BF),
    h2=((4, 128, 768), BF),
    dm=((4, 128, 768), BF),
    gb=((4, 128, 768), BF),
    du=((4, 128, 768), BF),
    xb=((2, 4, 128, 640), BF),
    pt=((3, 1024, 512), BF),
    vt=((2, 128, 1024), BF),
    kt=((2, 128, 1024), BF),
    back=((4, 128, 768), F32),
    ot=((2, 128, 512), F32),
    os=((4, 192, 128), BF),
    ob=((4, 192, 128), BF),
    o2=((4, 128, 128), BF),
    mms=((4, 128, 768), BF),
    mmr=((4, 128, 768), BF),
    dhs=((4, 128, 768), BF),
    dhr=((4, 128, 768), BF),
    das=((128, 768), BF),
    dos=((4, 192, 128), BF),
    dob=((4, 192, 128), BF),
    dst=((3, 1024, 512), BF),
    ga=((512, 640), F32),
    gps=((512, 512), BF),
    gpr=((512, 512), BF),
    dqkv=((4, 128, 768), BF),
    d1s=((4, 128, 768), BF),
    d1r=((4, 128, 768), BF),
    g_out=((4, 2, 96, 768), BF),
    g_in=((2, 4, 4, 48, 384), BF),
    g_attn=((2, 768, 384), BF),
    g_qkv=((2, 768, 384), BF),
    p_out=((4, 96, 768), BF),
    p_in=((4, 4, 48, 384), BF),
    p_attn=((768, 384), BF),
    p_qkv=((768, 384), BF),
    q_attn=((4, 192, 384), BF),
    q_qkv=((4, 192, 384), BF),
    m_attn=((192, 384), BF),
    m_qkv=((192, 384), BF),
    r_out=((4, 96, 768), BF),
    r_in=((4, 4, 48, 384), BF),
    via_in=((4, 48, 384), BF),
    via_out=((96, 768), BF),
    via_dh1=((128, 768), BF),
    m_in=((4, 48, 384), BF),
    u_in=((4, 48, 384), BF),
    r_attn=((4, 48, 384), BF),
    r_qkv=((4, 48, 384), BF),
    t_in=((4, 48, 384), F32),
    t_attn=((1, 48, 384), F32),
    t_qkv=((4, 48, 384), F32),
    f_in=((4, 2, 24, 384), F32),
    f_attn=((1, 2, 24, 384), F32),
    f_qkv=((4, 2, 24, 384), F32),
    early=((8, 768), F32),
    early_pair=((8, 768), F32),
    early_line=((4, 8, 384), F32),
    early_plane=((4, 8, 384), F32),
    early_all=((2, 4, 8, 384), F32),
    late=((4, 768), F32),
    late_pair=((4, 768), F32),
    late_line=((4, 4, 384), F32),
    late_plane=((4, 4, 384), F32),
    late_all=((2, 4, 4, 384), F32),
    sq=((32, 1, 128), F32),
)


def dot(left, right):
    return jnp.dot(left, right, preferred_element_type=F32)


def dot_nt(left, right):
    return lax.dot_general(left, right, (((1,), (1,)), ((), ())), preferred_element_type=F32)


def dot_tn(left, right):
    return lax.dot_general(left, right, (((0,), (0,)), ((), ())), preferred_element_type=F32)


def loop(count, body, start=0):
    def step(index, carry):
        body(index)
        return carry

    lax.fori_loop(start, count, step, 0)


def layer_kernel(
    i_time,
    i_start,
    i_len,
    h_tok,
    h_cot,
    h_vec,
    h_wada,
    h_wqkv,
    h_wattn,
    h_win,
    h_wout,
    o_y,
    o_dx,
    o_norm,
    o_gqkv,
    o_gattn,
    o_gin,
    o_gout,
    o_dmod,
    o_gvec,
    o_vec,
    o_conds,
    *scratch,
):
    r = SimpleNamespace(**dict(zip(SCRATCH, scratch)), when=scratch[-3])
    send_sems, recv_sems = scratch[-2:]
    i_tok, i_cot, i_vec, i_wada = r.i_tok, r.i_cot, r.i_vec, r.i_wada
    i_wqkv, i_wattn, i_win, i_wout = r.i_wqkv, r.i_wattn, r.i_win, r.i_wout
    b, s = lax.axis_index("dp"), lax.axis_index("seq")
    z, c = lax.div(s, 2), lax.rem(s, 2)
    mate = s + 1 - 2 * c
    chip = b * LINE + z
    me = b * SEQ + s
    drains = []

    def push(src, dst, at, to_b, to_s, out=None):
        pltpu.make_async_remote_copy(
            src_ref=src,
            dst_ref=dst,
            send_sem=send_sems.at[at if out is None else out],
            recv_sem=recv_sems.at[at],
            device_id=(to_b, to_s),
            device_id_type=MESH,
        ).start()

    def keep(src, dst, at):
        pltpu.make_async_copy(src, dst, recv_sems.at[at]).start()

    def got(at, like):
        pltpu.make_async_copy(like, like, recv_sems.at[at]).wait()

    def left(at, like):
        pltpu.make_async_copy(like, like, send_sems.at[at]).wait()

    def sent(at, like):
        drains.append(lambda: left(at, like))

    def by_core(body):
        for h, width in ((0, HALF), (1, PACK - HALF)):

            @pl.when(c == h)
            def _():
                body(slice(HALF * h, HALF * h + width), width)

    def sent_by_core(at, like):
        drains.append(lambda: by_core(lambda columns, width: left(at, like(width))))

    near = (b, b + 1 - 2 * lax.rem(b, 2), b + 2 - 4 * lax.div(b, 2), 3 - b)

    def toward(k):
        if k == 3:
            return 3, near[3]
        slot = 1 + c if k == 1 else 2 - c
        return slot, (1 - c) * near[k] + c * near[3 - k]

    def peers(body):
        for k in (1, 2, 3):
            body(*toward(k))

    def stack(body):
        for k in (1, 2, 3):
            body(lax.rem(z + k + 2 * c * (2 - k), LINE))

    def line_gather(block, at, near=True, rest=True):
        inner = 1 + lax.rem(z, 2)
        if near:
            push(block(z), block(z), at + z, b, 2 * inner + c, at)

        def one(to):
            relayed = ((z == 1) & (to == 3)) | ((z == 2) & (to == 0))

            @pl.when(jnp.logical_not(relayed | (to == inner)))
            def _():
                push(block(z), block(z), at + z, b, 2 * to + c, at)

        if rest:
            stack(one)

    def line_relay(block, at):
        for middle, source, to in ((2, 1, 3), (1, 2, 0)):

            @pl.when(z == middle)
            def _():
                got(at + source, block(source))
                push(block(source), block(source), at + source, b, 2 * to + c, at)

    def line_got(block, at, k):
        here = (k == z) | ((z == 2) & (k == 1)) | ((z == 1) & (k == 2))

        @pl.when(jnp.logical_not(here))
        def _():
            got(at + k, block(0))

    far = lax.div(z, 2)

    def line_order(j):
        return lax.rem(z + (2, 3 - 2 * far, 1 + 2 * far, 0)[j], LINE)

    def line_add(j, rows, dst, via, at):
        to = line_order(j)
        outer_chip = (z == 0) | (z == 3)

        def direct():
            push(rows(to), dst.at[z], at + z, b, 2 * to + c, at)

        if j == 0:

            @pl.when(outer_chip)
            def _():
                push(rows(to), via, at + 4, b, 2 * (1 + far) + c, at)

            @pl.when(jnp.logical_not(outer_chip))
            def _():
                direct()

        elif j < 3:
            direct()
        else:
            keep(rows(z), dst.at[z], at + z)

    def line_via(via, at, add):
        @pl.when((z == 1) | (z == 2))
        def _():
            got(at + 4, via)
            add()

    def line_done(dst, at):
        for k in range(4):
            missing = ((z == 1) & (k == 3)) | ((z == 2) & (k == 0))

            @pl.when(jnp.logical_not(missing))
            def _():
                got(at + k, dst.at[k])

    def line_clear(dst):
        for middle, k in ((1, 3), (2, 0)):

            @pl.when(z == middle)
            def _():
                dst[k] = jnp.zeros(dst.shape[1:], BF)

    lane = lax.broadcasted_iota(jnp.int32, (1, 128), 1)
    low = lane < 64
    own24 = pl.ds(pl.multiple_of(24 * c, 8), 24)
    mate24 = pl.ds(pl.multiple_of(24 * (1 - c), 8), 24)
    part = pl.ds(pl.multiple_of(HALF * c, 128), HALF)
    chip_rows = pl.ds(pl.multiple_of(48 * chip, 16), 48)
    group_rows = pl.ds(pl.multiple_of(192 * b, 16), 192)

    barrier = pltpu.get_barrier_semaphore()

    def greet(k):
        other = lax.rem(me + k, ALL)
        pl.semaphore_signal(
            barrier, inc=1, device_id=(lax.div(other, SEQ), lax.rem(other, SEQ)), device_id_type=MESH
        )

    loads = (
        (i_time, r.when.at[0]),
        (i_start, r.when.at[1]),
        (i_len, r.when.at[2]),
        (h_wqkv, i_wqkv),
        (h_win, i_win),
        (h_wattn, i_wattn),
        (h_wout, i_wout),
        (h_tok, i_tok),
        (h_vec, i_vec),
        (h_wada, i_wada),
        (h_cot, i_cot),
    )
    for k, (src, dst) in enumerate(loads):
        pltpu.make_async_copy(src, dst, recv_sems.at[S.load + k]).start()
    loop(ALL, greet, 1)
    for k, (src, dst) in enumerate(loads):
        pltpu.make_async_copy(src, dst, recv_sems.at[S.load + k]).wait()

    def natural(kind, p, head):
        return kind * WIDTH + 192 * p + 64 * head

    def half_at(ref, column, high):
        tile = ref[:, column // 128 * 128 : column // 128 * 128 + 128]
        return tile if (column % 128 == 64) == high else pltpu.roll(tile, 64, 1)

    for p in range(4):
        for tile in range(5):
            pair = []
            for high in (0, 1):
                which = HALVES[2 * tile + high]
                pair.append(
                    jnp.zeros((24, 128), F32)
                    if which is None
                    else half_at(i_wqkv, natural(which[0], p, which[1]), bool(high))
                )
            r.wide_qkv[own24, 768 * p + 128 * tile : 768 * p + 128 * tile + 128] = jnp.where(
                low, pair[0], pair[1]
            )
        r.wide_qkv[own24, 768 * p + 640 : 768 * p + 768] = jnp.zeros((24, 128), F32)
    r.wide_in[own24, :] = i_win[...]
    r.wide_attn[own24, :] = i_wattn[...]
    r.w_out[z, c] = i_wout[...].astype(BF)
    r.toks[z] = i_tok[0]
    line_clear(r.r_out)
    line_clear(r.r_in)
    line_clear(r.d1r)
    for ref in (r.q_qkv, r.r_qkv):
        ref[:, :, PACK - HALF : HALF] = jnp.zeros((4, ref.shape[1], WIDTH - PACK), BF)
    lanes8 = lax.broadcasted_iota(jnp.int32, (8, 128), 1)
    half_cond = COND // 2
    speed = jnp.exp((lanes8 % half_cond).astype(F32) * (-math.log(10000.0) / half_cond))
    angle = r.when[0, 0].astype(F32) * speed
    wave = jnp.where(lanes8 < half_cond, jnp.cos(angle), jnp.sin(angle))
    r.conds_all[b] = wave * (1.0 / (1.0 + jnp.exp(-wave)))
    pl.semaphore_wait(barrier, ALL - 1)

    def token_block(k):
        return r.toks.at[k]

    def attn_block(k):
        return r.w_attn.at[pl.ds(pl.multiple_of(192 * b + 48 * k, 16), 48), part]

    def in_block(k):
        return r.w_in.at[:, k, :, part]

    def out_block(k):
        return r.w_out.at[k, c]

    peers(lambda k, to: push(r.conds_all.at[b], r.conds_all.at[b], S.cond, to, s))
    sent(S.cond, r.conds_all.at[0:3])
    push(r.wide_qkv.at[own24], r.wide_qkv.at[own24], S.mix_qkv, b, mate)
    sent(S.mix_qkv, r.wide_qkv.at[0:24])
    push(r.wide_attn.at[own24], r.wide_attn.at[own24], S.mix_attn, b, mate)
    sent(S.mix_attn, r.wide_attn.at[0:24])
    push(r.wide_in.at[own24], r.wide_in.at[own24], S.mix_in, b, mate)
    sent(S.mix_in, r.wide_in.at[0:24])

    got(S.cond, r.conds_all.at[0:3])
    row8 = lax.broadcasted_iota(jnp.int32, (8, 128), 0)
    cond4 = jnp.zeros((8, 128), F32)
    for k in range(4):
        cond4 = jnp.where(row8 == k, r.conds_all[k], cond4)
    o_conds[...] = cond4
    wide = i_wada.shape[0]
    r.mod_pad[...] = jnp.zeros((8, 384), F32)
    r.mod_pad[:, 0:wide] = dot_nt(cond4.astype(BF), i_wada[...].astype(BF))
    columns = pltpu.roll(r.mod_pad[...], lax.rem(wide * me, 128), 1)
    for k in range(4):
        for t in range(3):
            r.mod_send[k, t : t + 1, :] = columns[k : k + 1, 128 * t : 128 * t + 128]
        r.mod_send[k, 3:4, :] = jnp.zeros((1, 128), F32)

    def send_mod(k):
        other = lax.rem(chip + k, CHIPS)
        ob = lax.div(other, LINE)
        push(r.mod_send.at[ob], r.mod_got.at[c, chip], S.mod, ob, 2 * lax.rem(other, LINE) + c)

    loop(CHIPS, send_mod, 1)
    sent(S.mod, r.mod_got.at[0, 0:15])
    keep(r.mod_send.at[b], r.mod_got.at[c, chip], S.mod)

    def block(src, first):
        return src.at[:, pl.ds(pl.multiple_of(first, 128), HALF)]

    def slices_along_line():
        def send(columns, width):
            def rows(to):
                first = pl.multiple_of(WIDTH * to + columns.start, 128)
                return r.s_qkv.at[:, pl.ds(first, width)]

            dst = r.w_qkv.at[chip_rows, columns]
            stack(lambda to: push(rows(to), dst, S.w_qkv, b, 2 * to + c))
            keep(rows(z), dst, S.w_qkv)

        by_core(send)
        sent_by_core(S.w_qkv, lambda width: r.w_qkv.at[0:144, 0:width])

    def over_plane(dst, at):
        rows = dst.at[group_rows, part]
        peers(lambda k, to: push(rows, rows, at + k, to, s))
        for k in (1, 2, 3):
            sent(at + k, dst.at[0:192, 0:HALF])

    def share(dst, at, onward):
        for k in range(4):
            rows = dst.at[pl.ds(pl.multiple_of(192 * near[k], 16), 192), part]
            if k:
                got(at + k, rows)
            push(rows, rows, onward, b, mate)
        sent(onward, dst.at[:, 0:HALF])

    def line_share(block, at, onward):
        for k in range(4):
            line_got(block, at, k)
            push(block(k), block(k), onward, b, mate)

    got(S.mix_qkv, r.wide_qkv.at[0:24])
    r.s_qkv[...] = r.wide_qkv[...].astype(BF)
    slices_along_line()
    line_gather(token_block, S.tok, rest=False)
    sent(S.tok, r.toks.at[0:3])
    got(S.mix_attn, r.wide_attn.at[0:24])
    r.s_attn[...] = r.wide_attn[...].astype(BF)

    def qkv_over_plane(columns, width):
        got(S.w_qkv, r.w_qkv.at[0:192, 0:width])
        rows = r.w_qkv.at[group_rows, columns]
        peers(lambda k, to: push(rows, rows, S.group_qkv + k, to, s))

    by_core(qkv_over_plane)
    for k in (1, 2, 3):
        sent_by_core(S.group_qkv + k, lambda width: r.w_qkv.at[0:192, 0:width])
    line_gather(token_block, S.tok, near=False)
    for h in range(2):

        @pl.when(c == h)
        def _():
            r.w_attn[chip_rows, 384 * h : 384 * h + 384] = r.s_attn[:, 384 * h : 384 * h + 384]

    line_gather(attn_block, S.w_attn)
    sent(S.w_attn, r.w_attn.at[0:144, 0:HALF])
    line_gather(out_block, S.w_out)
    sent(S.w_out, r.w_out.at[0:3, 0])
    got(S.mix_in, r.wide_in.at[0:24])
    r.s_in[...] = r.wide_in[...].astype(BF)
    peers(
        lambda k, to: push(
            block(r.s_in, WIDTH * to + HALF * c), r.w_in.at[b, z, :, part], S.plane_in, to, s
        )
    )
    keep(block(r.s_in, WIDTH * b + HALF * c), r.w_in.at[b, z, :, part], S.plane_in)
    sent(S.plane_in, r.w_in.at[0:3, 0, :, 0:HALF])

    def hidden_rows(k):
        place = (2 * k + c) * ROWS + lax.broadcasted_iota(jnp.int32, (ROWS, 1), 0)
        return (place >= r.when[1, 0]) & (place < r.when[1, 0] + r.when[2, 0])

    def first_norm(tokens, k):
        x0 = jnp.where(hidden_rows(k), i_vec[8:9, :], tokens.astype(F32))
        normed, inverse = normalize(x0)
        r.n1[k] = normed
        r.inv1[k] = jnp.broadcast_to(inverse, (ROWS, 128))
        return x0

    r.x0[...] = first_norm(i_tok[0], z)

    got(S.mod, r.mod_got.at[0])
    push(r.mod_got.at[c], r.mod_got.at[c], S.mod_pair, b, mate)
    sent(S.mod_pair, r.mod_got.at[0])
    got(S.mod_pair, r.mod_got.at[0])
    r.mod_flat[...] = jnp.zeros((40, 128), F32)
    for k in range(ALL):
        first = 9 * k // 8
        r.mod_flat[first : first + 3, :] += r.mod_got[k % 2, k // 2, 0:3, :]
    for k in range(6):
        row = jnp.concatenate(
            [r.mod_flat[6 * k + t : 6 * k + t + 1, :] for t in range(6)], axis=1
        )
        r.mod[k : k + 1, :] = row + i_vec[2 + k : 3 + k, :]

    def mod(k):
        return r.mod[k : k + 1, :]

    def vec(k):
        return i_vec[k : k + 1, :]

    r.h1[z] = (r.n1[z] * vec(0) * (1.0 + mod(1)) + mod(0)).astype(BF)
    r.dm[0] = (i_cot[0].astype(F32) * mod(5)).astype(BF)
    peers(lambda k, to: push(r.dm.at[0], r.dm.at[k], S.dm + k, to, s))
    for k in (1, 2, 3):
        sent(S.dm + k, r.dm.at[0])

    lanes = lax.broadcasted_iota(jnp.int32, (ROWS, 128), 1)
    first_half = lanes % HD < HD // 2
    speed = jnp.exp((lanes % (HD // 2)).astype(F32) * (-math.log(10000.0) / (HD // 2)))
    row = lax.broadcasted_iota(jnp.int32, (ROWS, 128), 0)

    def table(k):
        angle = ((2 * k + c) * ROWS + row).astype(F32) * speed
        r.turn[0, k] = jnp.cos(angle)
        sine = jnp.sin(angle)
        r.turn[1, k] = jnp.where(first_half, -sine, sine)

    loop(LINE, table)

    line_relay(token_block, S.tok)

    def qkv_share(columns, width):
        for k in range(4):
            rows = r.w_qkv.at[pl.ds(pl.multiple_of(192 * near[k], 16), 192), columns]
            if k:
                got(S.group_qkv + k, rows)
            push(rows, rows, S.fw_qkv, b, mate)

    by_core(qkv_share)
    sent_by_core(S.fw_qkv, lambda width: r.w_qkv.at[:, 0:width])
    by_core(lambda columns, width: got(S.fw_qkv, r.w_qkv.at[:, 0 : PACK - width]))
    for k in range(5):
        columns = slice(128 * k, 128 * k + 128)
        r.t_w_qkv[columns, :] = r.w_qkv[:, columns].T

    def turned(tile, sign, k):
        other = jnp.where(first_half, pltpu.roll(tile, 96, 1), pltpu.roll(tile, 32, 1))
        return tile * r.turn[0, k] + sign * (other * r.turn[1, k])

    def project(j):
        k = lax.rem(z + j, LINE)

        @pl.when(j > 0)
        def _():
            line_got(token_block, S.tok, k)
            first_norm(r.toks[k], k)
            r.h1[k] = (r.n1[k] * vec(0) * (1.0 + mod(1)) + mod(0)).astype(BF)

        x = dot(r.h1[k], r.w_qkv[:, 0:PACK])
        tiles = [x[:, 128 * t : 128 * t + 128] for t in range(5)]
        tiles[0] = turned(tiles[0], 1.0, k) * 0.125
        tiles[1] = jnp.where(low, turned(tiles[1], 1.0, k) * 0.125, tiles[1])
        tiles[2] = turned(tiles[2], 1.0, k)
        tiles[3] = turned(tiles[3], 1.0, k)
        for t in range(5):
            r.xb[0, k, :, 128 * t : 128 * t + 128] = tiles[t].astype(BF)
        push(r.xb.at[0, k], r.xb.at[1, k], S.xf + k, b, mate)

    loop(4, project)
    line_relay(attn_block, S.w_attn)
    for k in range(4):
        line_got(attn_block, S.w_attn, k)
    over_plane(r.w_attn, S.group_attn)
    for k in range(4):
        sent(S.xf + k, r.xb.at[0, 0])

    for k in range(6):
        columns = slice(128 * k, 128 * k + 128)
        r.t_h1[columns, :] = r.h1[:, :, columns].reshape(512, 128).T
    for k in range(4):
        got(S.xf + k, r.xb.at[0, 0])

    def tile_of(t):
        return r.xb[:, :, :, 128 * t : 128 * t + 128].reshape(1024, 128)

    heads = ((0, 2, 4, True, True), (0, 2, 4, False, False), (1, 3, 1, True, False))

    def queries(head, first, size):
        q_tile, _, _, q_low, _ = heads[head]
        q = r.xb[0, first : first + size, :, 128 * q_tile : 128 * q_tile + 128]
        return jnp.where(low if q_low else ~low, q.reshape(size * 128, 128), jnp.zeros((), BF))

    r.vt[0] = tile_of(4).T
    r.vt[1] = tile_of(1).T
    for half in range(2):
        at = slice(256 * half, 256 * half + 256)
        for head in range(3):
            scores = dot_nt(tile_of(heads[head][1]), queries(head, 2 * half, 2))
            weights = jnp.exp(scores - jnp.max(scores, axis=0, keepdims=True))
            weights = weights * (1.0 / jnp.sum(weights, axis=0, keepdims=True))
            weights = weights.astype(BF)
            r.pt[head, :, at] = weights
            out = dot(r.vt[head // 2], weights)
            if head == 0:
                r.ot[0, 0:64, at] = out[0:64]
            elif head == 1:
                r.ot[0, 64:128, at] = out[64:128]
            else:
                r.ot[1, 0:64, at] = out[64:128]
                r.ot[1, 64:128, at] = jnp.zeros((64, 256), F32)
        for k in (2 * half, 2 * half + 1):
            across = slice(128 * k, 128 * k + 128)
            r.os[k, 0:128, :] = r.ot[0, :, across].T.astype(BF)
            third = r.ot[1, 0:64, across]
            third = jnp.concatenate([third, pltpu.roll(third, 64, 1)], axis=0)
            r.os[k, 128:192, :] = third.T[0:64].astype(BF)
        for to in (2 * half, 2 * half + 1):

            @pl.when(z == to)
            def _():
                keep(r.os.at[to], r.ob.at[z], S.o)

            @pl.when(z != to)
            def _():
                push(r.os.at[to], r.ob.at[z], S.o, b, 2 * to + c)

        if half == 0:
            line_relay(out_block, S.w_out)

    sent(S.o, r.os.at[0:3])
    got(S.plane_in, r.w_in.at[:, 0, :, 0:HALF])
    line_gather(in_block, S.w_in)
    sent(S.w_in, r.w_in.at[0:3, :, :, 0:HALF])
    for k in range(2):
        r.kt[k] = tile_of(2 + k).T
    share(r.w_attn, S.group_attn, S.fw_attn)
    got(S.fw_attn, r.w_attn.at[:, 0:HALF])
    for p in range(4):
        first = 192 * p
        r.t_w_attn[:, 256 * p : 256 * p + 128] = r.w_attn[first : first + 128, :].T
        third = r.w_attn[first + 128 : first + 192, :]
        r.t_w_attn[:, 256 * p + 128 : 256 * p + 256] = jnp.concatenate(
            [third, jnp.zeros_like(third)], axis=0
        ).T
    got(S.o, r.ob)
    a = jnp.zeros((ROWS, WIDTH), F32)
    for p in range(4):
        third = r.ob[p, 128:192, :].astype(F32)
        third = jnp.concatenate([third, pltpu.roll(third, 64, 1)], axis=0)
        r.o2[p] = jnp.where(low, third, 0.0).astype(BF)
        a += dot(r.ob[p, 0:128, :], r.w_attn[192 * p : 192 * p + 128, :])
        a += dot(r.o2[p, :, 0:64], r.w_attn[192 * p + 128 : 192 * p + 192, :])
    r.a[...] = a
    x1 = r.x0[...] + mod(2) * a
    r.x1[...] = x1
    n2, inv2 = normalize(x1)
    r.n2[...] = n2
    r.inv2[...] = jnp.broadcast_to(inv2, (ROWS, 128))
    r.h2[0] = (n2 * vec(1) * (1.0 + mod(4)) + mod(3)).astype(BF)
    peers(lambda k, to: push(r.h2.at[0], r.h2.at[k], S.h2 + k, to, s))
    for k in (1, 2, 3):
        sent(S.h2 + k, r.h2.at[0])
    line_relay(in_block, S.w_in)
    line_share(out_block, S.w_out, S.fw_out)
    sent(S.fw_out, r.w_out.at[:, 0])
    got(S.fw_out, r.w_out.at[:, 0])

    for k in range(6):
        columns = slice(128 * k, 128 * k + 128)
        r.t_w_out[columns, :] = r.w_out[:, :, :, columns].reshape(WIDTH, 128).T

    def feed_back(k):
        @pl.when(k > 0)
        def _():
            got(S.dm + k, r.dm.at[0])

        r.back[k] = dot(r.dm[k], r.t_w_out[...])

    loop(4, feed_back)
    line_share(in_block, S.w_in, S.fw_in)
    sent(S.fw_in, r.w_in.at[:, :, :, 0:HALF])
    got(S.fw_in, r.w_in.at[:, :, :, 0:HALF])
    for k in range(6):
        columns = slice(128 * k, 128 * k + 128)
        r.t_w_in[columns, :] = r.w_in[:, :, :, columns].reshape(WIDTH, 128).T

    def feed(first, count):
        at = slice(first, first + count)
        size = count * ROWS
        u = dot(r.h2[at].reshape(size, WIDTH), r.w_in[...].reshape(WIDTH, WIDTH))
        slope = 0.7978845608028654
        cube = 0.044715
        t = jnp.tanh(slope * (u + cube * u * u * u))
        r.gb[at] = (0.5 * u * (1.0 + t)).astype(BF).reshape(count, ROWS, WIDTH)
        bend = 0.5 * (1.0 + t) + 0.5 * u * (1.0 - t * t) * (slope * (1.0 + 3.0 * cube * u * u))
        du = (r.back[at].reshape(size, WIDTH) * bend).astype(BF)
        r.du[at] = du.reshape(count, ROWS, WIDTH)
        r.dhs[at] = dot(du, r.t_w_in[...]).astype(BF).reshape(count, ROWS, WIDTH)

    feed(0, 1)
    for first, count in ((1, 2), (3, 1)):
        for k in range(first, first + count):
            got(S.h2 + k, r.h2.at[0])
        feed(first, count)
        for k in range(first, first + count):
            slot, to = toward(k)
            push(r.dhs.at[slot], r.dhr.at[slot], S.dh2, to, s)
    sent(S.dh2, r.dhs.at[0:3])
    def gather(own, others):
        total = own[0].astype(F32)
        for k in (1, 2, 3):
            total += others[k].astype(F32)
        return total

    for k in range(2):
        rows = slice(384 * k, 384 * k + 384)
        result = dot_tn(r.gb[:, :, rows].reshape(512, 384), r.dm[...].reshape(512, 768))
        r.g_out[2 * k : 2 * k + 2] = result.astype(BF).reshape(2, 2, 96, 768)
    push(r.g_out.at[:, 1 - c], r.p_out, S.pair_out, b, mate)
    sent(S.pair_out, r.p_out)

    def to_mate(grad, dst, at):
        push(grad.at[1 - c], dst, at, b, mate)
        sent(at, dst)

    def pair_sum(grad, pair, at):
        got(at, pair)
        grad[c] = (grad[c].astype(F32) + pair[...].astype(F32)).astype(BF)

    def plane_sum(grad, dst, at, packed=False):
        def send(columns, width):
            def rows(to):
                return grad.at[c, pl.ds(pl.multiple_of(192 * to, 16), 192), 0:width]

            peers(lambda k, to: push(rows(to), dst.at[k, :, 0:width], at, to, s))
            keep(rows(b), dst.at[0, :, 0:width], at)

        if packed:
            by_core(send)
            sent_by_core(at, lambda width: dst.at[0:3, :, 0:width])
        else:
            send(None, HALF)
            sent(at, dst.at[0:3])

    def line_sum(src, total, dst, first, at, packed=False):
        def send(columns, width):
            got(first, src.at[:, :, 0:width])
            total[...] = (
                (src[0].astype(F32) + src[1].astype(F32))
                + (src[2].astype(F32) + src[3].astype(F32))
            ).astype(BF)

            def rows(to):
                return total.at[pl.ds(pl.multiple_of(48 * to, 16), 48), 0:width]

            stack(lambda to: push(rows(to), dst.at[z, :, 0:width], at, b, 2 * to + c))
            keep(rows(z), dst.at[z, :, 0:width], at)

        if packed:
            by_core(send)
            sent_by_core(at, lambda width: dst.at[0:3, :, 0:width])
        else:
            send(None, HALF)
            sent(at, dst.at[0:3])

    def trade(total, final, at):
        push(total.at[:, mate24], final.at[:, c], at, b, mate)
        sent(at, final.at[:, 0])
        final[:, c] = total[:, own24, :]

    def in_product(k):
        rows = slice(384 * k, 384 * k + 384)
        result = dot_tn(r.h2[:, :, rows].reshape(512, 384), r.du[...].reshape(512, 768)).astype(BF)
        for h in range(2):
            r.g_in[h, 2 * k : 2 * k + 2] = result[:, 384 * h : 384 * h + 384].reshape(2, 4, 48, 384)

    in_product(0)

    got(S.pair_out, r.p_out)
    for k in range(4):
        r.g_out[k, c] = (r.g_out[k, c].astype(F32) + r.p_out[k].astype(F32)).astype(BF)

    def out_rows(k):
        return r.g_out.at[k, c]

    for j in (0, 1):
        line_add(j, out_rows, r.r_out, r.via_out, S.line_out)
    in_product(1)
    to_mate(r.g_in, r.p_in, S.pair_in)

    def add_out():
        k = line_order(2)
        r.g_out[k, c] = (r.g_out[k, c].astype(F32) + r.via_out[...].astype(F32)).astype(BF)

    got(S.dh2, r.dhr.at[0:3])
    dh = gather(r.dhs, r.dhr)
    n2 = r.n2[...]
    inv2 = r.inv2[:, 0:1]
    r.early[...] = jnp.zeros((8, 768), F32)
    r.early[2:3, :] = jnp.sum(dh, axis=0, keepdims=True)
    both = jnp.sum(dh * n2, axis=0, keepdims=True)
    r.early[3:4, :] = both * vec(1)
    r.early[0:1, :] = both * (1.0 + mod(4))
    grad = dh * ((1.0 + mod(4)) * vec(1))
    dx1 = i_cot[0].astype(F32) + norm_back(n2, inv2, grad)
    r.dx1[...] = dx1
    r.early[1:2, :] = jnp.sum(dx1 * r.a[...], axis=0, keepdims=True)
    r.das[...] = (dx1 * mod(2)).astype(BF)
    def make_do(to):
        columns = pl.ds(pl.multiple_of(256 * to, 256), 256)
        result = dot(r.das[...], r.t_w_attn[:, columns])
        r.dos[to, 0:128, :] = result[:, 0:128].astype(BF)
        third = result[:, 128:256]
        third = jnp.where(low, third[0:64], pltpu.roll(third[64:128], 64, 1))
        r.dos[to, 128:192, :] = third.astype(BF)

    def send_do(to):
        make_do(to)
        push(r.dos.at[to], r.dob.at[z], S.do, b, 2 * to + c)

    stack(send_do)
    make_do(z)
    keep(r.dos.at[z], r.dob.at[z], S.do)
    sent(S.do, r.dos.at[0:3])
    for t in range(3):
        at = slice(256 * t, 256 * t + 256)
        mm = dot(r.gb[...].reshape(512, WIDTH), r.w_out[:, :, :, at].reshape(WIDTH, 256))
        r.mms[:, :, at] = mm.astype(BF).reshape(4, ROWS, 256)
    peers(lambda k, to: push(r.mms.at[k], r.mmr.at[k], S.mm, to, s))
    sent(S.mm, r.mms.at[0:3])

    for p in range(4):
        for rows, left_side in (
            (slice(192 * p, 192 * p + 128), r.ob[p, 0:128, :]),
            (slice(192 * p + 128, 192 * p + 192), r.o2[p]),
        ):
            result = dot_tn(left_side, r.das[...])[0 : rows.stop - rows.start].astype(BF)
            r.g_attn[0, rows, :] = result[:, 0:HALF]
            r.g_attn[1, rows, :] = result[:, HALF:WIDTH]
    to_mate(r.g_attn, r.p_attn, S.pair_attn)

    def small_sum(src, pair, line, plane, whole, at):
        def first():
            push(src, pair, at, b, mate)
            sent(at, src)

        def second():
            got(at, pair)
            total = src[...] + pair[...]
            line[z] = (1 - c) * total[:, 0:HALF] + c * total[:, HALF:WIDTH]
            stack(lambda to: push(line.at[z], line.at[z], at + 1, b, 2 * to + c))
            sent(at + 1, line.at[0:3])

        def third():
            got(at + 1, line.at[0:3])
            plane[b] = (line[0] + line[1]) + (line[2] + line[3])
            peers(lambda k, to: push(plane.at[b], plane.at[b], at + 2, to, s))
            sent(at + 2, plane.at[0:3])

        def fourth():
            got(at + 2, plane.at[0:3])
            whole[c] = plane[...]
            push(plane, whole.at[c], at + 3, b, mate)
            sent(at + 3, plane)

        def rows(k):
            return jnp.concatenate([whole[0, k], whole[1, k]], axis=1)

        return first, second, third, fourth, rows

    early_steps = small_sum(
        r.early, r.early_pair, r.early_line, r.early_plane, r.early_all, S.early
    )
    late_steps = small_sum(r.late, r.late_pair, r.late_line, r.late_plane, r.late_all, S.late)

    pair_sum(r.g_in, r.p_in, S.pair_in)
    line_via(r.via_out, S.line_out, add_out)
    for j in (2, 3):
        line_add(j, out_rows, r.r_out, r.via_out, S.line_out)
    sent(S.line_out, r.r_out.at[0:3])

    def in_rows(k):
        return r.g_in.at[c, :, k]

    for j in (0, 1):
        line_add(j, in_rows, r.r_in, r.via_in, S.line_in)

    def add_in():
        k = line_order(2)
        r.g_in[c, :, k] = (r.g_in[c, :, k].astype(F32) + r.via_in[...].astype(F32)).astype(BF)

    pair_sum(r.g_attn, r.p_attn, S.pair_attn)
    plane_sum(r.g_attn, r.q_attn, S.plane_attn)

    got(S.do, r.dob)
    dot0 = r.dob[:, 0:128, :].reshape(512, 128)
    third = r.dob[:, 128:192, :].astype(F32).reshape(256, 128)
    other_rows = jnp.where(low, pltpu.roll(third, 64, 1), 0.0).reshape(4, 64, 128)
    third = jnp.where(low, third, 0.0).reshape(4, 64, 128)
    dot1 = jnp.concatenate([third, other_rows], axis=1).reshape(512, 128)
    zero = jnp.zeros((), BF)
    moved = pltpu.roll(dot1, 64, 1).astype(BF)
    grads = (jnp.where(low, dot0, zero), jnp.where(low, zero, dot0), moved)
    product = dot0.astype(F32).T * r.ot[0]
    deltas = (
        jnp.sum(product[0:64], axis=0, keepdims=True),
        jnp.sum(product[64:128], axis=0, keepdims=True),
        jnp.sum(dot1.T * r.ot[1], axis=0, keepdims=True),
    )
    for head in range(3):
        values = tile_of(heads[head][2])
        for half in range(2):
            at = slice(256 * half, 256 * half + 256)
            dp = dot_nt(values, grads[head][at])
            r.dst[head, :, at] = (
                r.pt[head, :, at].astype(F32) * (dp - deltas[head][:, at])
            ).astype(BF)

    def key_grads(rows):
        dk = [dot(r.dst[head, rows, :], queries(head, 0, 4)) for head in range(3)]
        dv = [dot(r.pt[head, rows, :], grads[head]) for head in range(3)]
        return (dv[2], dk[0] + dk[1], dk[2], dv[0] + dv[1])

    for t, tile in enumerate(key_grads(slice(512, 1024))):
        r.gps[:, 128 * t : 128 * t + 128] = tile.astype(BF)
    push(r.gps, r.gpr, S.gp, b, mate)
    sent(S.gp, r.gps)
    for t, tile in enumerate(key_grads(slice(0, 512))):
        r.ga[:, 128 * t + 128 : 128 * t + 256] = tile
    for half in range(2):
        at = slice(256 * half, 256 * half + 256)
        turned_q = [dot(r.kt[head // 2], r.dst[head, :, at]) for head in range(3)]
        top = jnp.concatenate([turned_q[0][0:64], turned_q[1][64:128]], axis=0)
        r.ga[at, 0:128] = top.T * 0.125
        r.ga[at, 128:256] += turned_q[2].T * 0.125
    line_via(r.via_in, S.line_in, add_in)
    for j in (2, 3):
        line_add(j, in_rows, r.r_in, r.via_in, S.line_in)
    sent(S.line_in, r.r_in.at[0:3])
    got(S.gp, r.gpr)

    def dh1_rows(k):
        return r.d1s.at[k]

    def back_turn(k):
        rows = pl.ds(pl.multiple_of(128 * k, 128), 128)
        tiles = [r.ga[rows, 0:128]] + [
            r.ga[rows, 128 * t : 128 * t + 128]
            + r.gpr[rows, 128 * t - 128 : 128 * t].astype(F32)
            for t in range(1, 5)
        ]
        tiles[0] = turned(tiles[0], -1.0, k)
        tiles[1] = jnp.where(low, turned(tiles[1], -1.0, k), tiles[1])
        tiles[2] = turned(tiles[2], -1.0, k)
        tiles[3] = turned(tiles[3], -1.0, k)
        for t in range(5):
            r.dqkv[k, :, 128 * t : 128 * t + 128] = tiles[t].astype(BF)
        r.dqkv[k, :, PACK:WIDTH] = jnp.zeros((128, 128), BF)

    back_turn(line_order(0))

    def unproject(j):
        k = line_order(j)
        partial_sum = dot(r.dqkv[k, :, 0:PACK], r.t_w_qkv[...])
        r.d1s[k] = partial_sum.astype(BF)
        if j == 2:

            def add():
                r.d1s[k] = (partial_sum + r.via_dh1[...].astype(F32)).astype(BF)

            line_via(r.via_dh1, S.dh1, add)
        line_add(j, dh1_rows, r.d1r, r.via_dh1, S.dh1)
        n = r.n1[k]
        e = partial_sum * ((1.0 + mod(1)) * vec(0))
        weight = jnp.where(hidden_rows(k), r.inv1[k][:, 0:1], 0.0)
        centred = (
            e
            - jnp.mean(e, axis=-1, keepdims=True)
            - n * jnp.mean(e * n, axis=-1, keepdims=True)
        )
        r.late[0:1, :] += jnp.sum(partial_sum * n, axis=0, keepdims=True)
        r.late[1:2, :] += jnp.sum(partial_sum, axis=0, keepdims=True)
        r.late[3:4, :] += jnp.sum(weight * centred, axis=0, keepdims=True)

    r.late[...] = jnp.zeros((4, 768), F32)
    r.late[3:4, :] = jnp.sum(
        jnp.where(hidden_rows(z), r.dx1[...], 0.0), axis=0, keepdims=True
    )
    unproject(0)
    for j in (1, 2, 3):
        back_turn(line_order(j))

    def qkv_rows(k):
        rows = pl.ds(pl.multiple_of(128 * k, 128), 128)
        result = dot(r.t_h1[rows, :], r.dqkv[...].reshape(512, WIDTH)).astype(BF)
        r.g_qkv[0, rows, :] = result[:, 0:HALF]
        r.g_qkv[1, rows, :] = result[:, HALF:WIDTH]

    loop(6, qkv_rows)
    to_mate(r.g_qkv, r.p_qkv, S.pair_qkv)
    unproject(1)
    pair_sum(r.g_qkv, r.p_qkv, S.pair_qkv)
    plane_sum(r.g_qkv, r.q_qkv, S.plane_qkv, True)
    got(S.mm, r.mmr.at[0:3])
    mm = gather(r.mms, r.mmr)
    o_y[...] = (r.x1[...] + mod(5) * mm).astype(BF)
    r.early[4:5, :] = jnp.sum(i_cot[0].astype(F32) * mm, axis=0, keepdims=True)
    early_steps[0]()
    unproject(2)
    unproject(3)
    sent(S.dh1, r.d1s.at[0:3])
    both = r.late[0:1, :]
    r.late[2:3, :] = both * vec(0)
    r.late[0:1, :] = both * (1.0 + mod(1))
    late_steps[0]()
    early_steps[1]()
    line_sum(r.q_attn, r.m_attn, r.r_attn, S.plane_attn, S.line_attn)
    late_steps[1]()

    line_done(r.r_in, S.line_in)
    r.m_in[...] = (
        (r.r_in[0].astype(F32) + r.r_in[1].astype(F32))
        + (r.r_in[2].astype(F32) + r.r_in[3].astype(F32))
    ).astype(BF)
    peers(lambda k, to: push(r.m_in.at[to], r.u_in.at[b], S.slice_in, to, s))
    keep(r.m_in.at[b], r.u_in.at[b], S.slice_in)
    sent(S.slice_in, r.u_in.at[0:3])
    line_sum(r.q_qkv, r.m_qkv, r.r_qkv, S.plane_qkv, S.line_qkv, True)
    early_steps[2]()
    late_steps[2]()

    line_done(r.d1r, S.dh1)
    dh = (r.d1r[0].astype(F32) + r.d1r[1].astype(F32)) + (
        r.d1r[2].astype(F32) + r.d1r[3].astype(F32)
    )
    n1 = r.n1[z]
    grad = dh * ((1.0 + mod(1)) * vec(0))
    dx0 = r.dx1[...] + norm_back(n1, r.inv1[z][:, 0:1], grad)
    o_dx[...] = jnp.where(hidden_rows(z), 0.0, dx0)
    early_steps[3]()
    late_steps[3]()

    line_done(r.r_out, S.line_out)
    total = (r.r_out[0].astype(F32) + r.r_out[1].astype(F32)) + (
        r.r_out[2].astype(F32) + r.r_out[3].astype(F32)
    )
    o_gout[...] = total
    squares = total * total
    squares = jnp.sum(squares[:, 0:128] + squares[:, 128:256] + squares[:, 256:384]
                      + squares[:, 384:512] + squares[:, 512:640] + squares[:, 640:768],
                      axis=0, keepdims=True)

    def fold(value):
        total = value[:, 0:128] * value[:, 0:128]
        for t in range(1, value.shape[1] // 128):
            total += value[:, 128 * t : 128 * t + 128] * value[:, 128 * t : 128 * t + 128]
        return jnp.sum(total, axis=0, keepdims=True)

    got(S.slice_in, r.u_in)
    r.t_in[...] = r.u_in[...].astype(F32)
    for p in range(4):
        squares += fold(r.t_in[p])
    trade(r.t_in, r.f_in, S.last_in)
    got(S.line_attn, r.r_attn)
    r.t_attn[0] = (r.r_attn[0].astype(F32) + r.r_attn[1].astype(F32)) + (
        r.r_attn[2].astype(F32) + r.r_attn[3].astype(F32)
    )
    squares += fold(r.t_attn[0])
    trade(r.t_attn, r.f_attn, S.last_attn)
    by_core(lambda columns, width: got(S.line_qkv, r.r_qkv.at[:, :, 0:width]))
    r.t_qkv[...] = r.r_qkv[...].astype(F32)
    trade(r.t_qkv, r.f_qkv, S.last_qkv)
    for p in range(4):
        squares += fold(r.t_qkv[p])
    r.sq[me] = squares

    def send_sq(k):
        other = lax.rem(me + k, ALL)
        push(r.sq.at[me], r.sq.at[me], S.sq, lax.div(other, SEQ), lax.rem(other, SEQ))

    loop(ALL, send_sq, 1)
    sent(S.sq, r.sq.at[0:31])
    got(S.last_in, r.f_in.at[:, 0])
    got(S.last_attn, r.f_attn.at[:, 0])
    for h in range(2):
        for p in range(4):
            value = r.f_in[p, h]
            o_gin[:, 768 * p + 384 * h : 768 * p + 384 * h + 384] = value
        value = r.f_attn[0, h]
        o_gattn[:, 384 * h : 384 * h + 384] = value
    got(S.last_qkv, r.f_qkv.at[:, 0])
    where = {which: index for index, which in enumerate(HALVES) if which is not None}

    def packed_half(chunk, high):
        kind, rest = chunk // 12, chunk % 12
        index = where[(kind, rest % 3)]
        t = index // 2
        tile = r.f_qkv[rest // 3, t // 3, :, t % 3 * 128 : t % 3 * 128 + 128]
        return tile if index % 2 == high else pltpu.roll(tile, 64, 1)

    for t in range(18):
        o_gqkv[:, 128 * t : 128 * t + 128] = jnp.where(
            low, packed_half(2 * t, 0), packed_half(2 * t + 1, 1)
        )
    got(S.early + 3, r.early_all.at[0])
    got(S.late + 3, r.late_all.at[0])
    early_rows = [early_steps[4](k) for k in range(4)]
    late_rows = [late_steps[4](k) for k in range(4)]
    mods = []
    for k in range(4):
        early, late = early_rows[k], late_rows[k]
        rows = jnp.concatenate([late[1:3], early[1:5], jnp.zeros((2, 768), F32)], axis=0)
        for n in range(6):
            for m in range(6):
                r.dmod_flat[k, 6 * n + m : 6 * n + m + 1, :] = rows[
                    n : n + 1, 128 * m : 128 * m + 128
                ]
        mods.append(rows)
    gain = jnp.concatenate(
        [
            sum(late_rows[k][0:1] for k in range(4)),
            sum(early_rows[k][0:1] for k in range(4)),
            (mods[0] + mods[1] + mods[2] + mods[3])[0:6],
        ],
        axis=0,
    )
    mask_row = sum(late_rows[k][3:4] for k in range(4))
    gains = jnp.concatenate([gain, mask_row, jnp.zeros((7, 768), F32)], axis=0)
    masters = jnp.concatenate([i_vec[...], jnp.zeros((7, 768), F32)], axis=0)
    own = lax.rem(WIDTH - 24 * me, WIDTH)
    o_gvec[...] = pltpu.roll(gains, own, 1)[:, 0:128]
    o_vec[...] = pltpu.roll(masters, own, 1)[:, 0:128]
    r.mod_pad[...] = jnp.zeros((8, 384), F32)
    window = lax.div(wide * me, 128)
    for k in range(4):
        rows = r.dmod_flat[k, pl.ds(window, 3), :]
        for m in range(3):
            r.mod_pad[k : k + 1, 128 * m : 128 * m + 128] = rows[m : m + 1, :]
    o_dmod[...] = pltpu.roll(r.mod_pad[...], lax.rem(384 - lax.rem(wide * me, 128), 384), 1)[:, 0:256]
    small = jnp.sum(gain * gain) + jnp.sum(mask_row * mask_row)
    conds = [r.conds_all[k][0:1].astype(BF).astype(F32) for k in range(4)]
    for k in range(4):
        for m in range(k, 4):
            term = jnp.sum(mods[k] * mods[m]) * jnp.sum(conds[k] * conds[m])
            small += term if m == k else 2.0 * term
    got(S.sq, r.sq.at[0:31])
    total = r.sq[0]
    for k in range(1, ALL):
        total += r.sq[k]
    o_norm[...] = jnp.broadcast_to(jnp.sqrt(jnp.sum(total) + small), (8, 128))

    for drained in drains:
        drained()


def run_layer(*args):
    shapes = (
        ((ROWS, WIDTH), BF),
        ((ROWS, WIDTH), F32),
        ((8, 128), F32),
        ((24, 3 * WIDTH), F32),
        ((24, WIDTH), F32),
        ((24, 4 * WIDTH), F32),
        ((96, WIDTH), F32),
        ((8, 256), F32),
        ((16, 128), F32),
        ((16, 128), F32),
        ((8, 128), F32),
    )
    whole = pl.BlockSpec(memory_space=pltpu.VMEM)
    return pl.pallas_call(
        layer_kernel,
        out_shape=[jax.ShapeDtypeStruct(shape, kind) for shape, kind in shapes],
        in_specs=[pl.BlockSpec(memory_space=pl.ANY)] * len(args),
        out_specs=[whole] * len(shapes),
        scratch_shapes=[pltpu.VMEM(shape, kind) for shape, kind in SCRATCH.values()]
        + [pltpu.SMEM((3, 1), jnp.int32)]
        + [pltpu.SemaphoreType.DMA((SEM_COUNT,)), pltpu.SemaphoreType.DMA((SEM_COUNT,))],
        compiler_params=pltpu.CompilerParams(
            collective_id=0, has_side_effects=True, vmem_limit_bytes=60 * 1024 * 1024
        ),
    )(*args)


HELD = (2, 8, 9, 7, 10, 3, 4, 5, 6)


def finish_kernel(*refs):
    sources, outs, refs = refs[:28], refs[28:49], refs[49:]
    near, results, load_sems, store_sems = refs[:28], refs[28:46], refs[46], refs[47]
    norm, g_vec, own_vec, dmod, conds = near[:5]
    weights, moments = (own_vec, *near[9:14]), near[14:26]

    order = list(range(5)) + [14, 15, 9, 16, 17]
    for k in (4, 5, 2, 3):
        order += [3 + k, 8 + k, 14 + 2 * k, 15 + 2 * k]
    loads = {}
    for n in (26, 27):
        loads[n] = pltpu.make_async_copy(sources[n - 26], near[n], load_sems.at[n])
        loads[n].start()
    for n in order:
        source = sources[HELD[n]] if n < 9 else sources[n + 2]
        loads[n] = pltpu.make_async_copy(source, near[n], load_sems.at[n])
        loads[n].start()
    for n in order[:10]:
        loads[n].wait()
    outs[2][0, 0] = norm[0, 0]
    clip = jnp.minimum(1.0, CLIP / (norm[0:1, 0:1] + 1e-06))
    wide, narrow = near[9].shape[0], moments[0].shape[1]
    rounded = conds[...].astype(BF).astype(F32)
    turned_mod = dmod[...].T
    g_ada = turned_mod[0:wide, 0:1] * rounded[0:1, :]
    for k in range(1, 4):
        g_ada += turned_mod[0:wide, k : k + 1] * rounded[k : k + 1, :]
    stores = []
    for n in (26, 27):
        loads[n].wait()
        stores.append(pltpu.make_async_copy(near[n], outs[n - 26].at[0], store_sems.at[n - 8]))
        stores[-1].start()
    for step, k in enumerate((0, 1, 4, 5, 2, 3)):
        if step > 1:
            for n in order[2 + 4 * step : 6 + 4 * step]:
                loads[n].wait()
        grad = g_vec[0:9, 0:narrow] if k == 0 else g_ada if k == 1 else near[3 + k][...]
        updated = adam_step(
            weights[k][...] if k else own_vec[0:9, 0:narrow],
            grad * clip,
            moments[2 * k][...],
            moments[2 * k + 1][...],
            RATE if k else RATE_VECTORS,
            DECAY if k else 0.0,
        )
        for n in range(3):
            at = 3 * k + n
            results[at][...] = updated[n]
            stores.append(pltpu.make_async_copy(results[at], outs[3 + at], store_sems.at[at]))
            stores[-1].start()
    for copy in stores:
        copy.wait()


def run_finish(partial_results, weights, moments):
    shapes = [((1, ROWS, WIDTH), BF), ((1, ROWS, WIDTH), F32), ((1, 1), F32)]
    for moment in moments[::2]:
        shapes += [(moment.shape, F32)] * 3
    far = pl.BlockSpec(memory_space=pl.ANY)
    specs = [far] * len(shapes)
    specs[2] = pl.BlockSpec(memory_space=pltpu.SMEM)
    near = [partial_results[k] for k in HELD] + [*weights, *moments, *partial_results[:2]]
    args = (*partial_results, *weights, *moments)
    return pl.pallas_call(
        finish_kernel,
        out_shape=[jax.ShapeDtypeStruct(shape, kind) for shape, kind in shapes],
        in_specs=[far] * len(args),
        out_specs=specs,
        scratch_shapes=[pltpu.VMEM(array.shape, array.dtype) for array in near]
        + [pltpu.VMEM(shape, kind) for shape, kind in shapes[3:]]
        + [pltpu.SemaphoreType.DMA((28,)), pltpu.SemaphoreType.DMA((20,))],
        compiler_params=pltpu.CompilerParams(vmem_limit_bytes=60 * 1024 * 1024),
    )(*args)


def slices(
    tokens_in,
    cotangent,
    timesteps,
    span_start,
    span_len,
    vectors,
    w_ada,
    w_qkv,
    w_attn,
    w_in,
    w_out,
    m_vec,
    v_vec,
    m_ada,
    v_ada,
    m_qkv,
    v_qkv,
    m_attn,
    v_attn,
    m_in,
    v_in,
    m_out,
    v_out,
):
    partial_results = run_layer(
        timesteps,
        span_start,
        span_len,
        tokens_in,
        cotangent,
        vectors,
        w_ada.T,
        w_qkv,
        w_attn,
        w_in,
        w_out,
    )
    moments = (
        m_vec,
        v_vec,
        m_ada.T,
        v_ada.T,
        m_qkv,
        v_qkv,
        m_attn,
        v_attn,
        m_in,
        v_in,
        m_out,
        v_out,
    )
    results = run_finish(partial_results, (w_ada.T, w_qkv, w_attn, w_in, w_out), moments)
    ada_results = [result.T for result in results[6:9]]
    return (*results[:2], results[2].reshape(()), *results[3:6], *ada_results, *results[9:])


def solution(mesh):
    in_specs = (
        P("dp", "seq", None),
        P("dp", "seq", None),
        P("dp"),
        P("dp"),
        P("dp"),
        P(),
        P(None, ("dp", "seq")),
        P(("dp", "seq"), None),
        P(("dp", "seq"), None),
        P(("dp", "seq"), None),
        P(("dp", "seq"), None),
        P(None, ("dp", "seq")),
        P(None, ("dp", "seq")),
        P(None, ("dp", "seq")),
        P(None, ("dp", "seq")),
        P(("dp", "seq"), None),
        P(("dp", "seq"), None),
        P(("dp", "seq"), None),
        P(("dp", "seq"), None),
        P(("dp", "seq"), None),
        P(("dp", "seq"), None),
        P(("dp", "seq"), None),
        P(("dp", "seq"), None),
    )
    out_specs = (
        P("dp", "seq", None),
        P("dp", "seq", None),
        P(),
        P(None, ("dp", "seq")),
        P(None, ("dp", "seq")),
        P(None, ("dp", "seq")),
        P(None, ("dp", "seq")),
        P(None, ("dp", "seq")),
        P(None, ("dp", "seq")),
        P(("dp", "seq"), None),
        P(("dp", "seq"), None),
        P(("dp", "seq"), None),
        P(("dp", "seq"), None),
        P(("dp", "seq"), None),
        P(("dp", "seq"), None),
        P(("dp", "seq"), None),
        P(("dp", "seq"), None),
        P(("dp", "seq"), None),
        P(("dp", "seq"), None),
        P(("dp", "seq"), None),
        P(("dp", "seq"), None),
    )
    sizes = dict(mesh.shape)
    local = slices if (sizes["dp"], sizes["seq"]) == (4, 8) else plain
    return jax.shard_map(local, mesh=mesh, in_specs=in_specs, out_specs=out_specs, check_vma=False)
```
